32 devices in a mesh: fsdp: 4 (over x, core), ctx: 2 (over y), tp: 4 (over z).
Axes of the slice: x: 2, y: 2, z: 4, core: 2. Of those that a mesh axis runs over, the one named last changes fastest.
Arguments:
- tokens: bfloat16 [16, 2048, 1024], P('fsdp', 'ctx'), may hold values from -6 to 6
- teacher: bfloat16 [16, 2048, 1024], P('fsdp', 'ctx'), may hold values from -12 to 12
- lengths: int32 [16], P('fsdp'), may hold values from 512 to 2048, as said below
- attn_gain: bfloat16 [1024], P('fsdp'), may hold values from 0.25 to 1.75
- q_weight: bfloat16 [1024, 1024], P('fsdp', 'tp'), may hold values from -0.1875 to 0.1875
- k_weight: bfloat16 [1024, 512], P('fsdp', 'tp'), may hold values from -0.1875 to 0.1875
- v_weight: bfloat16 [1024, 512], P('fsdp', 'tp'), may hold values from -0.1875 to 0.1875
- q_gain: bfloat16 [64], P('fsdp'), may hold values from 0.25 to 1.75
- k_gain: bfloat16 [64], P('fsdp'), may hold values from 0.25 to 1.75
- o_weight: bfloat16 [1024, 1024], P('tp', 'fsdp'), may hold values from -3 to 3
- ffn_gain: bfloat16 [1024], P('fsdp'), may hold values from 0.25 to 1.75
- gate_weight: bfloat16 [1024, 4608], P('fsdp', 'tp'), may hold values from -0.1875 to 0.1875
- up_weight: bfloat16 [1024, 4608], P('fsdp', 'tp'), may hold values from -0.1875 to 0.1875
- down_weight: bfloat16 [4608, 1024], P('tp', 'fsdp'), may hold values from -0.09375 to 0.09375
Outputs:
- output: bfloat16 [16, 2048, 1024], P('fsdp', 'ctx')
- teacher_loss: float32 [], replicated
- tokens_grad: float32 [16, 2048, 1024], P('fsdp', 'ctx')
- attn_gain_grad: float32 [1024], P('fsdp')
- q_weight_grad: float32 [1024, 1024], P('fsdp', 'tp')
- k_weight_grad: float32 [1024, 512], P('fsdp', 'tp')
- v_weight_grad: float32 [1024, 512], P('fsdp', 'tp')
- q_gain_grad: float32 [64], P('fsdp')
- k_gain_grad: float32 [64], P('fsdp')
- o_weight_grad: float32 [1024, 1024], P('tp', 'fsdp')
- ffn_gain_grad: float32 [1024], P('fsdp')
- gate_weight_grad: float32 [1024, 4608], P('fsdp', 'tp')
- up_weight_grad: float32 [1024, 4608], P('fsdp', 'tp')
- down_weight_grad: float32 [4608, 1024], P('tp', 'fsdp')
The draws below stay inside these ranges and needn't reach their ends.
Inputs may be any that keep to these rules, and one draw needn't show every extreme that they name: `lengths`: each row holds one sequence from slot 0; slots from its length on are padding. At least one row in every draw is full.
All inputs are finite; a program needn't handle non-finite values.
Results may differ from the reference program's by a relative error of at most 0.014.
Values may be sent and summed in bfloat16 or wider, within the bound.
A program may use at most 320 MiB of HBM per device.

```python
import jax
import jax.numpy as jnp
from jax import lax

D = 1024
HQ = 16
KV = 8
HD = 64
FF = 4608
ROW = 2048
ROWS = 16


def draw_lengths(key, part):
    key = jax.random.fold_in(key, 11)
    key_one, key_two = jax.random.split(key)
    drawn = jax.random.randint(key_one, (ROWS,), ROW // 4, ROW + 1)
    full_row = jax.random.randint(key_two, (), 0, ROWS)
    return jnp.where(jnp.arange(ROWS) == full_row, ROW, drawn).astype(jnp.int32)


def draw_teacher(key, part):
    key = jax.random.fold_in(key, 13)
    key_one, key_two = jax.random.split(key)
    row_place = jnp.arange(ROWS, dtype=jnp.float32) / max(ROWS - 1, 1)
    jitter = jnp.exp(jax.random.uniform(key_one, (ROWS,), jnp.float32, jnp.log(0.7), jnp.log(1.4)))
    base = 3.0 ** row_place
    noise = jnp.clip(jax.random.normal(key_two, (ROWS, ROW, D), jnp.float32), -2.8, 2.8)
    scale = (base * jitter)[:, None, None]
    return (noise * scale).astype(jnp.bfloat16)


def shard_levels(key, extent, pieces, least, high):
    def one(axis_at, parts):
        steps = jax.random.uniform(jax.random.fold_in(jax.random.fold_in(key, 6), axis_at), (parts,), jnp.float32, least / len(pieces), high / len(pieces))
        return jnp.repeat(jnp.exp(steps), extent[axis_at] // parts).reshape((-1,) + (1,) * (len(extent) - axis_at - 1))

    factor_of = one(*pieces[0])
    for cut in pieces[1:]:
        factor_of = factor_of * one(*cut)
    return factor_of


def bell_draw(own_key, shape, scale, reach, cuts=(), kind=jnp.bfloat16):
    values = scale * jax.random.normal(own_key, shape, jnp.float32)
    if cuts:
        values = values * shard_levels(own_key, shape, cuts, -0.22, 0.18)
    return jnp.clip(values, -reach, reach).astype(kind)


def setup_inputs(seed: int = 0) -> dict:
    streams_of = jax.random.split(jax.random.key(seed), 15)
    return {
        "tokens": bell_draw(streams_of[0], (ROWS, ROW, D), 1.0, 6.0, ((0, 4), (1, 2))),
        "teacher": draw_teacher(jax.random.fold_in(streams_of[14], 71), 0),
        "lengths": draw_lengths(jax.random.fold_in(streams_of[14], 71), 0),
        "attn_gain": jnp.clip(1.0 + 0.15 * jax.random.normal(streams_of[3], (D,), jnp.float32), 0.25, 1.75).astype(jnp.bfloat16),
        "q_weight": bell_draw(streams_of[4], (D, HQ * HD), D ** -0.5, 0.1875, ((0, 4), (1, 4))),
        "k_weight": bell_draw(streams_of[5], (D, KV * HD), D ** -0.5, 0.1875, ((0, 4), (1, 4))),
        "v_weight": bell_draw(streams_of[6], (D, KV * HD), D ** -0.5, 0.1875, ((0, 4), (1, 4))),
        "q_gain": jnp.clip(1.0 + 0.15 * jax.random.normal(streams_of[7], (HD,), jnp.float32), 0.25, 1.75).astype(jnp.bfloat16),
        "k_gain": jnp.clip(1.0 + 0.15 * jax.random.normal(streams_of[8], (HD,), jnp.float32), 0.25, 1.75).astype(jnp.bfloat16),
        "o_weight": bell_draw(streams_of[9], (HQ * HD, D), (HD // 16) ** -0.5, 3.0, ((0, 4), (1, 4))),
        "ffn_gain": jnp.clip(1.0 + 0.15 * jax.random.normal(streams_of[10], (D,), jnp.float32), 0.25, 1.75).astype(jnp.bfloat16),
        "gate_weight": bell_draw(streams_of[11], (D, FF), D ** -0.5, 0.1875, ((0, 4), (1, 4))),
        "up_weight": bell_draw(streams_of[12], (D, FF), D ** -0.5, 0.1875, ((0, 4), (1, 4))),
        "down_weight": bell_draw(streams_of[13], (FF, D), FF ** -0.5, 0.09375, ((0, 4), (1, 4))),
    }


EPS = 1e-05
THETA = 1000000.0
NEGATIVE = -1e+30
HIGH = lax.Precision.HIGHEST

@jax.custom_vjp
def low(v):
    return lax.optimization_barrier(v.astype(jnp.bfloat16)).astype(jnp.float32)

@jax.custom_vjp
def low_back(v):
    return v

def low_keep(v):
    return (low(v), None)

def low_pass(kept, grad):
    return (grad,)

def back_keep(v):
    return (v, None)

def back_low(kept, grad):
    return (low(grad),)
low.defvjp(low_keep, low_pass)
low_back.defvjp(back_keep, back_low)

def rms_scale(field_in, gain_vec):
    return field_in * lax.rsqrt(lax.optimization_barrier(jnp.mean(field_in * field_in, axis=-1, keepdims=True)) + EPS) * gain_vec

def rotate(field_in, positions):
    half_dim = field_in.shape[-1] // 2
    frequency = THETA ** (-(2.0 * jnp.arange(half_dim, dtype=jnp.float32)) / field_in.shape[-1])
    angles = positions[:, None] * frequency[None, :]
    cos_part = jnp.cos(angles)[:, None, :]
    sin_part = jnp.sin(angles)[:, None, :]
    lower_half = field_in[..., :half_dim]
    upper_half = field_in[..., half_dim:]
    return jnp.concatenate([lower_half * cos_part - upper_half * sin_part, upper_half * cos_part + lower_half * sin_part], axis=-1)

def product_full(left_mat, right_mat):
    return jnp.dot(left_mat, right_mat, precision=HIGH, preferred_element_type=jnp.float32)

def attend(queries, key_rows, values, length):
    group_size = HQ // KV
    query_len = min(ROW, 512)
    query_blocks = queries.reshape(ROW // query_len, query_len, KV, group_size, HD)
    block_starts = jnp.arange(ROW // query_len, dtype=jnp.int32) * query_len
    key_pos = jnp.arange(ROW, dtype=jnp.int32)
    score_scale = HD ** (-0.5)

    def one_block(block_args):
        query_block, block_start = block_args
        query_pos = block_start + jnp.arange(query_len, dtype=jnp.int32)
        scores = low_back(score_scale * jnp.einsum('qhgd,khd->hgqk', query_block, key_rows, precision=HIGH))
        allowed = (key_pos[None, :] <= query_pos[:, None]) & (key_pos[None, :] < length)
        scores = jnp.where(allowed, scores, NEGATIVE)
        probs_low = low(jax.nn.softmax(scores, axis=-1))
        return jnp.einsum('hgqk,khd->qhgd', probs_low, values, precision=HIGH)
    mixed = lax.map(jax.checkpoint(one_block), (query_blocks, block_starts))
    return mixed.reshape(ROW, HQ * HD)

def row_forward(weights, row_input, row_teacher, length):
    gain_one, w_query, w_key, w_value, gain_query, gain_key, w_output, gain_two, w_gate, w_upper, w_down = weights
    slot_pos = jnp.arange(ROW, dtype=jnp.int32)
    positions = slot_pos.astype(jnp.float32)
    normed_one = low(rms_scale(row_input, gain_one))
    query_raw = low_back(product_full(normed_one, w_query)).reshape(ROW, HQ, HD)
    key_raw = low_back(product_full(normed_one, w_key)).reshape(ROW, KV, HD)
    values = low(low_back(product_full(normed_one, w_value))).reshape(ROW, KV, HD)
    queries = low(rotate(rms_scale(query_raw, gain_query), positions))
    key_rows = low(rotate(rms_scale(key_raw, gain_key), positions))
    attended = low(low_back(attend(queries, key_rows, values, length)))
    resid = row_input + low_back(product_full(attended, w_output))
    normed_two = low(rms_scale(resid, gain_two))
    gate_act = low_back(product_full(normed_two, w_gate))
    up_act = low_back(product_full(normed_two, w_upper))
    hidden = low(jax.nn.silu(gate_act) * up_act)
    result = resid + low_back(product_full(hidden, w_down))
    valid = (slot_pos < length).astype(jnp.float32)[:, None]
    error_value = result - row_teacher
    return (result, jnp.sum(valid * error_value * error_value))

def reference(tokens, teacher, lengths, attn_gain, q_weight, k_weight, v_weight, q_gain, k_gain, o_weight, ffn_gain, gate_weight, up_weight, down_weight):
    weights = tuple((item.astype(jnp.float32) for item in (attn_gain, q_weight, k_weight, v_weight, q_gain, k_gain, o_weight, ffn_gain, gate_weight, up_weight, down_weight)))
    inputs = tokens.astype(jnp.float32)
    targets = teacher.astype(jnp.float32)
    valid_count = jnp.sum(lengths).astype(jnp.float32)

    def forward(inputs, weights):

        def one_row(row_args):
            row_input, row_teacher, length = row_args
            return row_forward(weights, row_input, row_teacher, length)
        results, squares = lax.map(jax.checkpoint(one_row), (inputs, targets, lengths))
        return (results, jnp.sum(squares) / (valid_count * D))
    (results, teacher_loss), backward = jax.vjp(forward, inputs, weights)
    loss_weight = jnp.asarray(0.5 * ROWS * ROW * D, dtype=jnp.float32)
    grad_inputs, grad_weights = backward((jnp.zeros_like(results), loss_weight))
    return (results.astype(jnp.bfloat16), teacher_loss, grad_inputs, grad_weights[0], grad_weights[1], grad_weights[2], grad_weights[3], grad_weights[4], grad_weights[5], grad_weights[6], grad_weights[7], grad_weights[8], grad_weights[9], grad_weights[10])
```

```python
import functools
import math

import jax
import jax.numpy as jnp
from jax import lax
from jax.experimental import pallas as pl
from jax.experimental.pallas import tpu as pltpu
from jax.sharding import PartitionSpec as P

EPS = 1e-05
THETA = 1000000.0
NEGATIVE = -1e30


def rms_scale(field_in, gain_vec):
    return (
        field_in * lax.rsqrt(jnp.mean(field_in * field_in, axis=-1, keepdims=True) + EPS) * gain_vec
    )


def rotate(field_in, positions):
    half_dim = field_in.shape[-1] // 2
    frequency = THETA ** (-(2.0 * jnp.arange(half_dim, dtype=jnp.float32)) / field_in.shape[-1])
    angles = positions[:, None] * frequency[None, :]
    cos_part = jnp.cos(angles)[:, None, :]
    sin_part = jnp.sin(angles)[:, None, :]
    lower_half = field_in[..., :half_dim]
    upper_half = field_in[..., half_dim:]
    return jnp.concatenate(
        [
            lower_half * cos_part - upper_half * sin_part,
            upper_half * cos_part + lower_half * sin_part,
        ],
        axis=-1,
    )


def linear(left_mat, right_mat):
    return jnp.dot(left_mat, right_mat, preferred_element_type=jnp.float32)


def linear_left(left_mat, right_mat):
    return lax.dot_general(
        left_mat, right_mat, (((0,), (0,)), ((), ())), preferred_element_type=jnp.float32
    )


def linear_right(left_mat, right_mat):
    return lax.dot_general(
        left_mat, right_mat, (((1,), (1,)), ((), ())), preferred_element_type=jnp.float32
    )


def swiglu(gate_act, up_act):
    return jax.nn.silu(gate_act) * up_act


def per_device_any(
    tokens,
    teacher,
    lengths,
    attn_gain,
    q_weight,
    k_weight,
    v_weight,
    q_gain,
    k_gain,
    o_weight,
    ffn_gain,
    gate_weight,
    up_weight,
    down_weight,
):
    (
        gain_one,
        w_query,
        w_key,
        w_value,
        gain_query,
        gain_key,
        w_output,
        gain_two,
        w_gate,
        w_upper,
        w_down,
    ) = (
        lax.all_gather(attn_gain, "fsdp", axis=0, tiled=True),
        lax.all_gather(q_weight, "fsdp", axis=0, tiled=True),
        lax.all_gather(k_weight, "fsdp", axis=0, tiled=True),
        lax.all_gather(v_weight, "fsdp", axis=0, tiled=True),
        lax.all_gather(q_gain, "fsdp", axis=0, tiled=True),
        lax.all_gather(k_gain, "fsdp", axis=0, tiled=True),
        lax.all_gather(o_weight, "fsdp", axis=1, tiled=True),
        lax.all_gather(ffn_gain, "fsdp", axis=0, tiled=True),
        lax.all_gather(gate_weight, "fsdp", axis=0, tiled=True),
        lax.all_gather(up_weight, "fsdp", axis=0, tiled=True),
        lax.all_gather(down_weight, "fsdp", axis=1, tiled=True),
    )
    rows_dev, block_len, model_width = tokens.shape
    count_tok = rows_dev * block_len
    head_dim = gain_query.shape[0]
    q_heads = w_query.shape[1] // head_dim
    kv_heads = w_key.shape[1] // head_dim
    group_size = q_heads // kv_heads
    score_scale = head_dim ** (-0.5)
    row_len = block_len * lax.axis_size("ctx")
    key_block = math.gcd(row_len, 512)
    block_start = lax.axis_index("ctx") * block_len
    tiles_used = (block_start + block_len + key_block - 1) // key_block
    slot_pos = block_start + jnp.arange(block_len, dtype=jnp.int32)
    positions = slot_pos.astype(jnp.float32)
    valid = (slot_pos[None, :] < lengths[:, None]).astype(jnp.float32)
    slots = count_tok * lax.axis_size("fsdp") * lax.axis_size("ctx")
    gain_two_f = gain_two.astype(jnp.float32)
    gain_one_f = gain_one.astype(jnp.float32)
    inputs = tokens.astype(jnp.float32)
    normed_one, back_one = jax.vjp(rms_scale, inputs, gain_one_f)
    normed_low = normed_one.astype(jnp.bfloat16).reshape(count_tok, model_width)
    query_raw = linear(normed_low, w_query)
    key_raw = linear(normed_low, w_key)
    value_raw = linear(normed_low, w_value)

    def heads_post(raw_heads, gain_vec):
        shaped = raw_heads.reshape(rows_dev, block_len, -1, head_dim)
        return rotate(rms_scale(shaped, gain_vec), positions)

    query_rot, query_back = jax.vjp(heads_post, query_raw, gain_query.astype(jnp.float32))
    key_rot, key_back = jax.vjp(heads_post, key_raw, gain_key.astype(jnp.float32))
    queries = query_rot.astype(jnp.bfloat16).reshape(
        rows_dev, block_len, kv_heads, group_size, head_dim
    )
    key_rows = key_rot.astype(jnp.bfloat16).reshape(rows_dev, block_len, kv_heads * head_dim)
    values = value_raw.astype(jnp.bfloat16).reshape(rows_dev, block_len, kv_heads * head_dim)
    keys_all, values_all = (
        lax.all_gather(key_rows, "ctx", axis=1, tiled=True),
        lax.all_gather(values, "ctx", axis=1, tiled=True),
    )

    def key_tile(tile_index):
        tile_start = tile_index * key_block
        key_pos = tile_start + jnp.arange(key_block, dtype=jnp.int32)
        key_part = lax.dynamic_slice_in_dim(keys_all, tile_start, key_block, 1).reshape(
            rows_dev, key_block, kv_heads, head_dim
        )
        value_part = lax.dynamic_slice_in_dim(values_all, tile_start, key_block, 1).reshape(
            rows_dev, key_block, kv_heads, head_dim
        )
        scores = (
            jnp.einsum("rqhgd,rkhd->rhgqk", queries, key_part, preferred_element_type=jnp.float32)
            * score_scale
        )
        allowed = (key_pos[None, None, :] <= slot_pos[None, :, None]) & (
            key_pos[None, None, :] < lengths[:, None, None]
        )
        return (tile_start, scores, allowed[:, None, None], key_part, value_part)

    stat_shape = (rows_dev, kv_heads, group_size, block_len)

    def stats_step(tile_index, carried):
        running_max, running_sum = carried
        tile_start, scores, allowed, key_part, value_part = key_tile(tile_index)
        masked = jnp.where(allowed, scores, NEGATIVE)
        new_max = jnp.maximum(running_max, jnp.max(masked, axis=-1))
        terms = jnp.where(allowed, jnp.exp(masked - new_max[..., None]), 0.0)
        return (new_max, running_sum * jnp.exp(running_max - new_max) + jnp.sum(terms, axis=-1))

    running_max, running_sum = lax.fori_loop(
        0,
        tiles_used,
        stats_step,
        (jnp.full(stat_shape, NEGATIVE, jnp.float32), jnp.zeros(stat_shape, jnp.float32)),
    )
    log_total = running_max + jnp.log(running_sum)
    out_shape = (rows_dev, block_len, kv_heads, group_size, head_dim)

    def value_step(tile_index, carried):
        rounded_out, exact_out = carried
        tile_start, scores, allowed, key_part, value_part = key_tile(tile_index)
        tile_probs = jnp.where(allowed, jnp.exp(scores - log_total[..., None]), 0.0)
        rounded_out = rounded_out + jnp.einsum(
            "rhgqk,rkhd->rqhgd",
            tile_probs.astype(jnp.bfloat16),
            value_part,
            preferred_element_type=jnp.float32,
        )
        exact_out = exact_out + jnp.einsum(
            "rhgqk,rkhd->rqhgd", tile_probs, value_part.astype(jnp.float32)
        )
        return (rounded_out, exact_out)

    rounded_out, exact_out = lax.fori_loop(
        0,
        tiles_used,
        value_step,
        (jnp.zeros(out_shape, jnp.float32), jnp.zeros(out_shape, jnp.float32)),
    )
    attended = rounded_out.astype(jnp.bfloat16).reshape(count_tok, q_heads * head_dim)
    attn_total = lax.psum(linear(attended, w_output), "tp")
    resid = inputs + attn_total.reshape(rows_dev, block_len, model_width)
    normed_two, back_two = jax.vjp(rms_scale, resid, gain_two_f)
    normed_second = normed_two.astype(jnp.bfloat16).reshape(count_tok, model_width)
    gate_act = linear(normed_second, w_gate)
    up_act = linear(normed_second, w_upper)
    hidden_full, back_glu = jax.vjp(swiglu, gate_act, up_act)
    hidden = hidden_full.astype(jnp.bfloat16)
    ffn_total = lax.psum(linear(hidden, w_down), "tp")
    result = resid + ffn_total.reshape(rows_dev, block_len, model_width)
    error_value = result - teacher.astype(jnp.float32)
    valid_col = valid[..., None]
    total_square, total_count = lax.psum(
        (jnp.sum(valid_col * error_value * error_value), jnp.sum(valid)), ("fsdp", "ctx")
    )
    teacher_loss = total_square / (total_count * model_width)
    grad_result = valid_col * error_value * (slots / total_count)
    grad_low = grad_result.astype(jnp.bfloat16).reshape(count_tok, model_width)
    grad_down = linear_left(hidden, grad_low)
    grad_hidden = linear_right(grad_low, w_down)
    grad_gate_full, grad_up_full = back_glu(grad_hidden)
    grad_gate = grad_gate_full.astype(jnp.bfloat16)
    grad_up = grad_up_full.astype(jnp.bfloat16)
    grad_wgate = linear_left(normed_second, grad_gate)
    grad_wup = linear_left(normed_second, grad_up)
    normed_two_part = linear_right(grad_gate, w_gate) + linear_right(grad_up, w_upper)
    grad_normed_two = lax.psum(normed_two_part, "tp")
    grad_resid_norm, grad_gain_two = back_two(
        grad_normed_two.reshape(rows_dev, block_len, model_width)
    )
    grad_resid = grad_result + grad_resid_norm
    grad_attn_low = grad_resid.astype(jnp.bfloat16).reshape(count_tok, model_width)
    grad_woutput = linear_left(attended, grad_attn_low)
    grad_attended = linear_right(grad_attn_low, w_output).astype(jnp.bfloat16).reshape(out_shape)
    delta = jnp.einsum("rqhgd,rqhgd->rhgq", grad_attended.astype(jnp.float32), exact_out)
    full_shape = (rows_dev, row_len, kv_heads * head_dim)

    def grad_step(tile_index, carried):
        grad_queries, grad_keys, grad_values = carried
        tile_start, scores, allowed, key_part, value_part = key_tile(tile_index)
        tile_probs = jnp.where(allowed, jnp.exp(scores - log_total[..., None]), 0.0)
        grad_probs = jnp.einsum(
            "rqhgd,rkhd->rhgqk", grad_attended, value_part, preferred_element_type=jnp.float32
        )
        grad_scores = (tile_probs * (grad_probs - delta[..., None])).astype(jnp.bfloat16)
        grad_queries = (
            grad_queries
            + jnp.einsum(
                "rhgqk,rkhd->rqhgd", grad_scores, key_part, preferred_element_type=jnp.float32
            )
            * score_scale
        )
        key_term = (
            jnp.einsum(
                "rhgqk,rqhgd->rkhd", grad_scores, queries, preferred_element_type=jnp.float32
            )
            * score_scale
        )
        value_term = jnp.einsum(
            "rhgqk,rqhgd->rkhd",
            tile_probs.astype(jnp.bfloat16),
            grad_attended,
            preferred_element_type=jnp.float32,
        )
        grad_keys = lax.dynamic_update_slice_in_dim(
            grad_keys, key_term.reshape(rows_dev, key_block, kv_heads * head_dim), tile_start, 1
        )
        grad_values = lax.dynamic_update_slice_in_dim(
            grad_values, value_term.reshape(rows_dev, key_block, kv_heads * head_dim), tile_start, 1
        )
        return (grad_queries, grad_keys, grad_values)

    grad_queries, grad_keys, grad_values = lax.fori_loop(
        0,
        tiles_used,
        grad_step,
        (
            jnp.zeros(out_shape, jnp.float32),
            jnp.zeros(full_shape, jnp.float32),
            jnp.zeros(full_shape, jnp.float32),
        ),
    )
    key_grad, value_grad = (
        lax.psum_scatter(grad_keys, "ctx", scatter_dimension=1, tiled=True),
        lax.psum_scatter(grad_values, "ctx", scatter_dimension=1, tiled=True),
    )
    grad_query_raw, grad_gain_query = query_back(
        grad_queries.reshape(rows_dev, block_len, q_heads, head_dim)
    )
    grad_key_raw, grad_gain_key = key_back(
        key_grad.reshape(rows_dev, block_len, kv_heads, head_dim)
    )
    query_low = grad_query_raw.astype(jnp.bfloat16)
    key_low = grad_key_raw.astype(jnp.bfloat16)
    value_low = value_grad.reshape(count_tok, kv_heads * head_dim).astype(jnp.bfloat16)
    grad_wquery = linear_left(normed_low, query_low)
    grad_wkey = linear_left(normed_low, key_low)
    grad_wvalue = linear_left(normed_low, value_low)
    normed_part = (
        linear_right(query_low, w_query)
        + linear_right(key_low, w_key)
        + linear_right(value_low, w_value)
    )
    grad_normed_one, grad_gain_query, grad_gain_key = lax.psum(
        (normed_part, grad_gain_query, grad_gain_key), "tp"
    )
    grad_input_norm, grad_gain_one = back_one(
        grad_normed_one.reshape(rows_dev, block_len, model_width)
    )
    tokens_grad = grad_resid + grad_input_norm
    partials = (
        grad_gain_one,
        grad_wquery,
        grad_wkey,
        grad_wvalue,
        grad_gain_query,
        grad_gain_key,
        grad_woutput,
        grad_gain_two,
        grad_wgate,
        grad_wup,
        grad_down,
    )
    pieces = (
        lax.psum_scatter(partials[0], ("fsdp", "ctx"), scatter_dimension=0, tiled=True),
        lax.psum_scatter(partials[1], ("fsdp", "ctx"), scatter_dimension=0, tiled=True),
        lax.psum_scatter(partials[2], ("fsdp", "ctx"), scatter_dimension=0, tiled=True),
        lax.psum_scatter(partials[3], ("fsdp", "ctx"), scatter_dimension=0, tiled=True),
        lax.psum_scatter(partials[4], ("fsdp", "ctx"), scatter_dimension=0, tiled=True),
        lax.psum_scatter(partials[5], ("fsdp", "ctx"), scatter_dimension=0, tiled=True),
        lax.psum_scatter(partials[6], ("fsdp", "ctx"), scatter_dimension=1, tiled=True),
        lax.psum_scatter(partials[7], ("fsdp", "ctx"), scatter_dimension=0, tiled=True),
        lax.psum_scatter(partials[8], ("fsdp", "ctx"), scatter_dimension=0, tiled=True),
        lax.psum_scatter(partials[9], ("fsdp", "ctx"), scatter_dimension=0, tiled=True),
        lax.psum_scatter(partials[10], ("fsdp", "ctx"), scatter_dimension=1, tiled=True),
    )
    summed = (
        lax.all_gather(pieces[0], "ctx", axis=0, tiled=True),
        lax.all_gather(pieces[1], "ctx", axis=0, tiled=True),
        lax.all_gather(pieces[2], "ctx", axis=0, tiled=True),
        lax.all_gather(pieces[3], "ctx", axis=0, tiled=True),
        lax.all_gather(pieces[4], "ctx", axis=0, tiled=True),
        lax.all_gather(pieces[5], "ctx", axis=0, tiled=True),
        lax.all_gather(pieces[6], "ctx", axis=1, tiled=True),
        lax.all_gather(pieces[7], "ctx", axis=0, tiled=True),
        lax.all_gather(pieces[8], "ctx", axis=0, tiled=True),
        lax.all_gather(pieces[9], "ctx", axis=0, tiled=True),
        lax.all_gather(pieces[10], "ctx", axis=1, tiled=True),
    )
    return (
        result.astype(jnp.bfloat16),
        teacher_loss,
        tokens_grad,
        summed[0],
        summed[1],
        summed[2],
        summed[3],
        summed[4],
        summed[5],
        summed[6],
        summed[7],
        summed[8],
        summed[9],
        summed[10],
    )


BF16 = jnp.bfloat16
F32 = jnp.float32
LOG2E = math.log2(math.e)
X_SWAP = [(0, 2), (2, 0), (1, 3), (3, 1)]
CORE_SWAP = [(0, 1), (1, 0), (2, 3), (3, 2)]
Y_SWAP = [(0, 1), (1, 0)]
Z_UP = [(0, 1), (1, 2), (2, 3), (3, 0)]
Z_DOWN = [(0, 3), (1, 0), (2, 1), (3, 2)]


def fits(mesh):
    return dict(mesh.shape) == {"fsdp": 4, "ctx": 2, "tp": 4}


def dot(left, right, left_dim, right_dim):
    return lax.dot_general(
        left, right, (((left_dim,), (right_dim,)), ((), ())), preferred_element_type=F32
    )


def sigmoid(v):
    return 0.5 * jnp.tanh(0.5 * v) + 0.5


def attn_fwd_kernel(width, len_ref, q_ref, k_ref, v_ref, o_ref, lse_ref, key_rows):
    block = pl.program_id(1)
    slots = k_ref.shape[1]
    hd = k_ref.shape[0]
    scale = hd**-0.5 * LOG2E
    length = len_ref[0]

    @pl.when(block == 0)
    def _():
        pos = lax.broadcasted_iota(jnp.int32, (hd, slots), 1)
        row = lax.broadcasted_iota(jnp.int32, (hd, slots), 0)
        bias = jnp.where((row == 0) & (pos >= length), NEGATIVE, 0.0)
        both = jnp.concatenate([k_ref[...].astype(F32), bias], axis=0)
        key_rows[...] = both.T.astype(BF16)

    one_row = jnp.where(lax.broadcasted_iota(jnp.int32, (hd, 2 * width), 0) == 0, 1.0, 0.0)
    pair = jnp.concatenate([q_ref[:hd, :], q_ref[hd:, :]], axis=1)
    query = jnp.concatenate([pair, one_row.astype(BF16)], axis=0)

    def tile(start, carried, diagonal):
        out, total = carried
        scores = dot(key_rows[pl.ds(start, width), :], query, 1, 0)
        if diagonal:
            key_pos = lax.broadcasted_iota(jnp.int32, (width, width), 0)
            query_pos = lax.broadcasted_iota(jnp.int32, (width, width), 1)
            allowed = key_pos <= query_pos
            scores = jnp.where(jnp.concatenate([allowed, allowed], axis=1), scores, NEGATIVE)
        probs = jnp.exp2(scores * scale)
        total = total + jnp.sum(probs, axis=0, keepdims=True)
        out = out + dot(v_ref[:, pl.ds(start, width)], probs.astype(BF16), 1, 0)
        return out, total

    carried = (jnp.zeros((hd, 2 * width), F32), jnp.zeros((1, 2 * width), F32))
    full = jnp.minimum(block, lax.div(length + width - 1, width))
    carried = lax.fori_loop(
        0, full, lambda j, c: tile(pl.multiple_of(j * width, width), c, False), carried
    )
    out, total = tile(pl.multiple_of(block * width, width), carried, True)
    out = out * (1.0 / total)
    o_ref[:hd, :] = out[:, :width].astype(BF16)
    o_ref[hd:, :] = out[:, width:].astype(BF16)
    log_total = jnp.log2(total)
    lse_ref[0, 0:1, :] = log_total[:, :width]
    lse_ref[0, 1:2, :] = log_total[:, width:]


def attn_fwd(length, queries, keys, values, hd, width):
    kv_heads, slots = keys.shape[0] // hd, keys.shape[1]
    return pl.pallas_call(
        functools.partial(attn_fwd_kernel, width),
        grid=(kv_heads, slots // width),
        in_specs=[
            pl.BlockSpec(memory_space=pltpu.SMEM),
            pl.BlockSpec((2 * hd, width), lambda h, i: (h, i)),
            pl.BlockSpec((hd, slots), lambda h, i: (h, 0)),
            pl.BlockSpec((hd, slots), lambda h, i: (h, 0)),
        ],
        out_specs=[
            pl.BlockSpec((2 * hd, width), lambda h, i: (h, i)),
            pl.BlockSpec((1, 2, width), lambda h, i: (h, 0, i)),
        ],
        out_shape=[
            jax.ShapeDtypeStruct((kv_heads * 2 * hd, slots), BF16),
            jax.ShapeDtypeStruct((kv_heads, 2, slots), F32),
        ],
        scratch_shapes=[pltpu.VMEM((slots, 2 * hd), BF16)],
        compiler_params=pltpu.CompilerParams(
            dimension_semantics=("arbitrary", "arbitrary"), vmem_limit_bytes=40 << 20
        ),
        cost_estimate=pl.CostEstimate(
            flops=kv_heads * 2 * slots * slots * 256 * 2,
            bytes_accessed=8 * kv_heads * hd * slots * 2,
            transcendentals=kv_heads * slots * slots,
        ),
        name="attn_fwd",
    )(length, queries, keys, values)


def attn_bwd_kernel(
    width,
    len_ref,
    q_ref,
    k_ref,
    v_ref,
    o_ref,
    do_ref,
    lse_ref,
    dq_ref,
    dk_ref,
    dv_ref,
    key_rows,
    value_rows,
    key_sum,
    value_sum,
):
    block = pl.program_id(1)
    slots = k_ref.shape[1]
    hd = k_ref.shape[0]
    scale = hd**-0.5
    length = len_ref[0]

    @pl.when(block == 0)
    def _():
        pos = lax.broadcasted_iota(jnp.int32, (hd, slots), 1)
        row = lax.broadcasted_iota(jnp.int32, (hd, slots), 0)
        bias = jnp.where((row == 0) & (pos >= length), NEGATIVE, 0.0)
        both = jnp.concatenate([k_ref[...].astype(F32), bias], axis=0)
        key_rows[...] = both.T.astype(BF16)
        value_rows[...] = v_ref[...].astype(F32).T.astype(BF16)
        key_sum[...] = jnp.zeros_like(key_sum)
        value_sum[...] = jnp.zeros_like(value_sum)

    @pl.when(block * width < length)
    def _():
        one_row = jnp.where(lax.broadcasted_iota(jnp.int32, (hd, 2 * width), 0) == 0, 1.0, 0.0)
        pair = jnp.concatenate([q_ref[:hd, :], q_ref[hd:, :]], axis=1)
        query = jnp.concatenate([pair, one_row.astype(BF16)], axis=0)
        grad = jnp.concatenate([do_ref[:hd, :], do_ref[hd:, :]], axis=1)
        out = jnp.concatenate([o_ref[:hd, :], o_ref[hd:, :]], axis=1)
        query_rows = pair.astype(F32).T.astype(BF16)
        grad_rows = grad.astype(F32).T.astype(BF16)
        lse = jnp.concatenate([lse_ref[0, 0:1, :], lse_ref[0, 1:2, :]], axis=1)
        delta = jnp.sum(grad.astype(F32) * out.astype(F32), axis=0, keepdims=True)

        def tile(start, query_sum, diagonal):
            scores = dot(key_rows[pl.ds(start, width), :], query, 1, 0)
            if diagonal:
                key_pos = lax.broadcasted_iota(jnp.int32, (width, width), 0)
                query_pos = lax.broadcasted_iota(jnp.int32, (width, width), 1)
                allowed = key_pos <= query_pos
                scores = jnp.where(jnp.concatenate([allowed, allowed], axis=1), scores, NEGATIVE)
            probs = jnp.exp2(scores * (scale * LOG2E) - lse)
            grad_probs = dot(value_rows[pl.ds(start, width), :], grad, 1, 0)
            grad_scores = (probs * (grad_probs - delta)).astype(BF16)
            value_sum[pl.ds(start, width), :] += dot(probs.astype(BF16), grad_rows, 1, 0)
            key_sum[pl.ds(start, width), :] += dot(grad_scores, query_rows, 1, 0)
            return query_sum + dot(k_ref[:, pl.ds(start, width)], grad_scores, 1, 0)

        query_sum = lax.fori_loop(
            0,
            block,
            lambda j, s: tile(pl.multiple_of(j * width, width), s, False),
            jnp.zeros((hd, 2 * width), F32),
        )
        query_sum = tile(pl.multiple_of(block * width, width), query_sum, True) * scale
        dq_ref[:hd, :] = query_sum[:, :width].astype(BF16)
        dq_ref[hd:, :] = query_sum[:, width:].astype(BF16)

    @pl.when(block * width >= length)
    def _():
        dq_ref[...] = jnp.zeros_like(dq_ref)

    @pl.when(block == pl.num_programs(1) - 1)
    def _():
        dk_ref[...] = (key_sum[...] * scale).T.astype(BF16)
        dv_ref[...] = value_sum[...].T.astype(BF16)


def attn_bwd(length, queries, keys, values, out, grad, lse, hd, width):
    kv_heads, slots = keys.shape[0] // hd, keys.shape[1]
    pair_spec = pl.BlockSpec((2 * hd, width), lambda h, i: (h, i))
    head_spec = pl.BlockSpec((hd, slots), lambda h, i: (h, 0))
    return pl.pallas_call(
        functools.partial(attn_bwd_kernel, width),
        grid=(kv_heads, slots // width),
        in_specs=[
            pl.BlockSpec(memory_space=pltpu.SMEM),
            pair_spec,
            head_spec,
            head_spec,
            pair_spec,
            pair_spec,
            pl.BlockSpec((1, 2, width), lambda h, i: (h, 0, i)),
        ],
        out_specs=[pair_spec, head_spec, head_spec],
        out_shape=[
            jax.ShapeDtypeStruct((kv_heads * 2 * hd, slots), BF16),
            jax.ShapeDtypeStruct((kv_heads * hd, slots), BF16),
            jax.ShapeDtypeStruct((kv_heads * hd, slots), BF16),
        ],
        scratch_shapes=[
            pltpu.VMEM((slots, 2 * hd), BF16),
            pltpu.VMEM((slots, hd), BF16),
            pltpu.VMEM((slots, hd), F32),
            pltpu.VMEM((slots, hd), F32),
        ],
        compiler_params=pltpu.CompilerParams(
            dimension_semantics=("arbitrary", "arbitrary"), vmem_limit_bytes=40 << 20
        ),
        cost_estimate=pl.CostEstimate(
            flops=kv_heads * 5 * slots * slots * 256 * 2,
            bytes_accessed=14 * kv_heads * hd * slots * 2,
            transcendentals=kv_heads * slots * slots,
        ),
        name="attn_bwd",
    )(length, queries, keys, values, out, grad, lse)


def ffn_fwd_kernel(x_ref, wa_ref, wb_ref, in_ref, out_ref, act_ref, hid_ref):
    half = wa_ref.shape[0]
    units = wa_ref.shape[1] // 3
    x = x_ref[...]
    act = dot(x[:, :half], wa_ref[:, : 2 * units], 1, 0)
    act = act + dot(x[:, half:], wb_ref[:, : 2 * units], 1, 0)
    gate, upper = act[:, :units], act[:, units:]
    hidden = (gate * sigmoid(gate) * upper).astype(BF16)
    act_ref[...] = act.astype(BF16)
    hid_ref[...] = hidden
    out_ref[:, :half] = in_ref[:, :half] + dot(hidden, wa_ref[:, 2 * units :], 1, 1)
    out_ref[:, half:] = in_ref[:, half:] + dot(hidden, wb_ref[:, 2 * units :], 1, 1)


def ffn_fwd(x, w_a, w_b, total, tile):
    tok, width = x.shape
    cols = w_a.shape[1]
    units = cols // 3
    rows_of = lambda n: pl.BlockSpec((tile, n), lambda i: (i, 0))
    whole = lambda a: pl.BlockSpec(a.shape, lambda i: (0, 0), pipeline_mode=pl.Buffered(1))
    return pl.pallas_call(
        ffn_fwd_kernel,
        grid=(tok // tile,),
        in_specs=[rows_of(width), whole(w_a), whole(w_b), rows_of(width)],
        out_specs=[rows_of(width), rows_of(2 * units), rows_of(units)],
        out_shape=[
            jax.ShapeDtypeStruct((tok, width), F32),
            jax.ShapeDtypeStruct((tok, 2 * units), BF16),
            jax.ShapeDtypeStruct((tok, units), BF16),
        ],
        input_output_aliases={3: 0},
        compiler_params=pltpu.CompilerParams(
            dimension_semantics=("arbitrary",), vmem_limit_bytes=48 << 20
        ),
        cost_estimate=pl.CostEstimate(
            flops=2 * tok * width * cols, bytes_accessed=16 << 20, transcendentals=tok * units
        ),
        name="ffn_fwd",
    )(x, w_a, w_b, total)


def ffn_bwd_kernel(
    steps,
    grad_ref,
    act_ref,
    hid_ref,
    wa_ref,
    wb_ref,
    in_ref,
    xt_ref,
    gradt_ref,
    out_ref,
    keep_ref,
    send_ref,
    dact_all,
    hid_all,
):
    step = pl.program_id(0)
    half = wa_ref.shape[0]
    units = wa_ref.shape[1] // 3
    tile = grad_ref.shape[0]

    @pl.when(step < steps)
    def _():
        rows = pl.ds(pl.multiple_of(step * tile, tile), tile)
        grad = grad_ref[...]
        grad_hidden = dot(grad[:, :half], wa_ref[:, 2 * units :], 1, 0)
        grad_hidden = grad_hidden + dot(grad[:, half:], wb_ref[:, 2 * units :], 1, 0)
        gate = act_ref[:, :units].astype(F32)
        upper = act_ref[:, units:].astype(F32)
        sig = sigmoid(gate)
        silu = gate * sig
        dact_all[rows, :units] = (grad_hidden * upper * (sig + silu - silu * sig)).astype(BF16)
        dact_all[rows, units:] = (grad_hidden * silu).astype(BF16)
        hid_all[rows, :] = hid_ref[...]
        dact = dact_all[rows, :]
        out_ref[:, :half] = in_ref[:, :half] + dot(dact, wa_ref[:, : 2 * units], 1, 1)
        out_ref[:, half:] = in_ref[:, half:] + dot(dact, wb_ref[:, : 2 * units], 1, 1)

    def weight_rows(target):
        target[:, : 2 * units] = dot(xt_ref[...], dact_all[...], 1, 0).astype(BF16)
        target[:, 2 * units :] = dot(gradt_ref[...], hid_all[...], 1, 0).astype(BF16)

    @pl.when((step >= steps) & (step < steps + 2))
    def _():
        weight_rows(send_ref)

    @pl.when(step >= steps + 2)
    def _():
        weight_rows(keep_ref)


def ffn_bwd(grad, act, hidden, w_a, w_b, total, xt, gradt, tile):
    tok, width = grad.shape
    half, cols = w_a.shape
    units = cols // 3
    steps = tok // tile
    quarter = width // 4
    rows_of = lambda n: pl.BlockSpec((tile, n), lambda i: (jnp.minimum(i, steps - 1), 0))
    whole = lambda a: pl.BlockSpec(a.shape, lambda i: (0, 0), pipeline_mode=pl.Buffered(1))
    feature = lambda i: (jnp.where(i < steps + 2, jnp.maximum(i - steps, 0) + 2, i - steps - 2), 0)
    return pl.pallas_call(
        functools.partial(ffn_bwd_kernel, steps),
        grid=(steps + 4,),
        in_specs=[
            rows_of(width),
            rows_of(2 * units),
            rows_of(units),
            whole(w_a),
            whole(w_b),
            rows_of(width),
            pl.BlockSpec((quarter, tok), feature),
            pl.BlockSpec((quarter, tok), feature),
        ],
        out_specs=[
            rows_of(width),
            pl.BlockSpec((quarter, cols), lambda i: (jnp.maximum(i - steps - 2, 0), 0)),
            pl.BlockSpec((quarter, cols), lambda i: (jnp.clip(i - steps, 0, 1), 0)),
        ],
        out_shape=[
            jax.ShapeDtypeStruct((tok, width), F32),
            jax.ShapeDtypeStruct((half, cols), BF16),
            jax.ShapeDtypeStruct((half, cols), BF16),
        ],
        scratch_shapes=[pltpu.VMEM((tok, 2 * units), BF16), pltpu.VMEM((tok, units), BF16)],
        input_output_aliases={5: 0},
        compiler_params=pltpu.CompilerParams(
            dimension_semantics=("arbitrary",), vmem_limit_bytes=56 << 20
        ),
        cost_estimate=pl.CostEstimate(
            flops=4 * tok * width * cols, bytes_accessed=32 << 20, transcendentals=tok * units
        ),
        name="ffn_bwd",
    )(grad, act, hidden, w_a, w_b, total, xt, gradt)


def z_gather(block):
    one = lax.ppermute(block, "tp", Z_UP)
    three = lax.ppermute(block, "tp", Z_DOWN)
    two = lax.ppermute(one, "tp", Z_UP)
    return [block, one, two, three]


def plane_gather(block):
    half = block.shape[0] // 2
    first = lax.ppermute(block[:half], "fsdp", X_SWAP)
    second = lax.ppermute(first, "ctx", Y_SWAP)
    mine = jnp.concatenate([block, first, second], axis=0)
    return mine, lax.ppermute(mine, "fsdp", CORE_SWAP)


def add_low(left, right):
    return (left.astype(F32) + right.astype(F32)).astype(BF16)


def plane_reduce(keep, send, x_first):
    mine = add_low(keep, lax.ppermute(send, "fsdp", CORE_SWAP))
    q = mine.shape[0] // 4
    if x_first:
        own = add_low(mine[: 2 * q], lax.ppermute(mine[2 * q :], "fsdp", X_SWAP))
        return add_low(own[:q], lax.ppermute(own[q:], "ctx", Y_SWAP))
    other = jnp.concatenate([mine[q : 2 * q], mine[3 * q :]], axis=0)
    here = jnp.concatenate([mine[:q], mine[2 * q : 3 * q]], axis=0)
    here = add_low(here, lax.ppermute(other, "ctx", Y_SWAP))
    return add_low(here[:q], lax.ppermute(here[q:], "fsdp", X_SWAP))


def z_reduce(parts):
    two = add_low(parts[1], lax.ppermute(parts[2], "tp", Z_DOWN))
    total = parts[0].astype(F32) + lax.ppermute(two, "tp", Z_DOWN).astype(F32)
    return total + lax.ppermute(parts[3], "tp", Z_UP).astype(F32)


def per_device_rows(
    tokens,
    teacher,
    lengths,
    attn_gain,
    q_weight,
    k_weight,
    v_weight,
    q_gain,
    k_gain,
    o_weight,
    ffn_gain,
    gate_weight,
    up_weight,
    down_weight,
):
    z = lax.axis_index("tp")
    ctx = lax.axis_index("ctx")
    fsdp = lax.axis_index("fsdp")
    rows_dev, tok, width = tokens.shape
    lane = width // 8
    place = fsdp * 2 + ctx
    hd = q_gain.shape[0] * 4
    q_cols, k_cols = q_weight.shape[1], k_weight.shape[1]
    units = gate_weight.shape[1]
    row_len = tok * 2
    slots = rows_dev * 4 * row_len

    def pick(array, blocks):
        parts = [lax.dynamic_slice_in_dim(array, b * lane, lane, array.ndim - 1) for b in blocks]
        return jnp.concatenate(parts, axis=-1)

    def reorder(array):
        return pick(array, [jnp.bitwise_xor(j, place) for j in (0, 1, 4, 5, 2, 3, 6, 7)])

    def restore(array):
        away = [jnp.bitwise_xor(j, place) for j in range(8)]
        return pick(array, [(a & 1) + (a & 2) * 2 + (a & 4) // 2 for a in away])

    def half_order(block):
        half = block.shape[0] // 2
        return jnp.where(ctx == 0, block, jnp.concatenate([block[half:], block[:half]], axis=0))

    length = lax.dynamic_slice_in_dim(lengths, z, 1, 0)
    total_count = lax.psum(jnp.sum(lengths), "fsdp").astype(F32)
    gains = lax.all_gather(
        jnp.concatenate([attn_gain, ffn_gain, q_gain, k_gain]), "fsdp", axis=0, tiled=False
    ).astype(F32)
    quarter = width // 4
    gain_one = reorder(gains[:, :quarter].reshape(1, width))
    gain_two = reorder(gains[:, quarter : 2 * quarter].reshape(1, width))
    gain_query = gains[:, 2 * quarter : 2 * quarter + hd // 4].reshape(1, hd, 1)
    gain_key = gains[:, 2 * quarter + hd // 4 :].reshape(1, hd, 1)

    w_attn = half_order(jnp.concatenate([q_weight, k_weight, v_weight, o_weight.T], axis=1))
    w_ffn = half_order(jnp.concatenate([gate_weight, up_weight, down_weight.T], axis=1))
    attn_halves = [plane_gather(b) for b in z_gather(w_attn)]
    ffn_halves = [plane_gather(b) for b in z_gather(w_ffn)]
    proj = q_cols + 2 * k_cols
    w_proj = [jnp.concatenate([a[:, :proj], b[:, :proj]], axis=0) for a, b in attn_halves]
    w_proj = jnp.concatenate(w_proj, axis=1)
    w_out = [jnp.concatenate([a[:, proj:], b[:, proj:]], axis=0) for a, b in attn_halves]
    w_out = jnp.concatenate(w_out, axis=1)

    x_in = reorder(lax.dynamic_index_in_dim(tokens, z, 0, keepdims=False)).astype(F32)
    rho_one = lax.rsqrt(jnp.mean(x_in * x_in, axis=-1, keepdims=True) + EPS)
    normed_one = (x_in * rho_one * gain_one).astype(BF16)
    raw = dot(w_proj, normed_one, 0, 1).reshape(4, proj // hd, hd, tok)
    heads_q, heads_k = q_cols // hd, k_cols // hd
    raw_q = raw[:, :heads_q]
    raw_k = raw[:, heads_q : heads_q + heads_k]

    pos = (ctx * tok + jnp.arange(tok, dtype=jnp.int32)).astype(F32)
    frequency = THETA ** (-(2.0 * jnp.arange(hd // 2, dtype=F32)) / hd)
    angles = frequency[:, None] * pos[None, :]
    cos_part, sin_part = jnp.cos(angles), jnp.sin(angles)

    def turn(v, sin_part):
        a, b = v[..., : hd // 2, :], v[..., hd // 2 :, :]
        return jnp.concatenate(
            [a * cos_part - b * sin_part, b * cos_part + a * sin_part], axis=-2
        )

    def head_norm(v):
        return lax.rsqrt(jnp.mean(v * v, axis=-2, keepdims=True) + EPS)

    rho_q, rho_k = head_norm(raw_q), head_norm(raw_k)
    rot_q = turn(raw_q * rho_q * gain_query, sin_part).astype(BF16)
    rot_k = turn(raw_k * rho_k * gain_key, sin_part).astype(BF16)
    heads = jnp.concatenate([rot_q, rot_k, raw[:, heads_q + heads_k :].astype(BF16)], axis=1)

    def split_heads(v):
        return (
            lax.dynamic_slice_in_dim(v, ctx * 2, 2, 0),
            lax.dynamic_slice_in_dim(v, 2 - ctx * 2, 2, 0),
        )

    def to_rows(v):
        mine, theirs = split_heads(v)
        got = lax.ppermute(theirs, "ctx", Y_SWAP)
        return jnp.concatenate(
            [jnp.where(ctx == 0, mine, got), jnp.where(ctx == 0, got, mine)], axis=-1
        )

    rows = to_rows(heads)
    queries = rows[:, :heads_q].reshape(2 * q_cols, row_len)
    keys = rows[:, heads_q : heads_q + heads_k].reshape(2 * k_cols, row_len)
    values = rows[:, heads_q + heads_k :].reshape(2 * k_cols, row_len)
    attn_out, lse = attn_fwd(length, queries, keys, values, hd, 512)

    def to_slots(v):
        mine = lax.dynamic_slice_in_dim(v, ctx * tok, tok, v.ndim - 1)
        theirs = lax.dynamic_slice_in_dim(v, tok - ctx * tok, tok, v.ndim - 1)
        got = lax.ppermute(theirs, "ctx", Y_SWAP)
        return jnp.concatenate(
            [jnp.where(ctx == 0, mine, got), jnp.where(ctx == 0, got, mine)], axis=0
        )

    attended = to_slots(attn_out)
    resid = x_in + dot(attended, w_out, 0, 1)
    rho_two = lax.rsqrt(jnp.mean(resid * resid, axis=-1, keepdims=True) + EPS)
    normed_two = (resid * rho_two * gain_two).astype(BF16)

    result = resid
    acts, hiddens = [None] * 4, [None] * 4
    for k in (0, 1, 3, 2):
        result, acts[k], hiddens[k] = ffn_fwd(normed_two, *ffn_halves[k], result, 256)
    result_low = result.astype(BF16)

    def spread(v):
        parts = z_gather(restore(v))
        out = jnp.zeros((rows_dev, tok, width), v.dtype)
        for k in range(4):
            out = lax.dynamic_update_slice(out, parts[k][None], (lax.rem(z - k + 4, 4), 0, 0))
        return out

    output = spread(result_low)

    teach = reorder(lax.dynamic_index_in_dim(teacher, z, 0, keepdims=False)).astype(F32)
    valid = (ctx * tok + jnp.arange(tok, dtype=jnp.int32) < length[0]).astype(F32)[:, None]
    error = valid * (result - teach)
    square = lax.psum(jnp.sum(error * error), ("fsdp", "ctx", "tp"))
    teacher_loss = square / (total_count * width)
    grad_result = error * (slots / total_count)
    grad_low = grad_result.astype(BF16)

    normed_two_t, grad_low_t = normed_two.T, grad_low.T
    grad_two = jnp.zeros((tok, width), F32)
    ffn_parts = [None] * 4
    for k in (2, 1, 3, 0):
        grad_two, keep, send = ffn_bwd(
            grad_low,
            acts[k],
            hiddens[k],
            *ffn_halves[k],
            grad_two,
            normed_two_t,
            grad_low_t,
            256,
        )
        ffn_parts[k] = plane_reduce(keep, send, k in (1, 2))

    def norm_back(grad, value, rho, gain):
        scaled = grad * gain
        return rho * scaled - value * (
            rho * rho * rho * jnp.mean(scaled * value, axis=-1, keepdims=True)
        )

    grad_gain_two = jnp.sum(grad_two * resid * rho_two, axis=0, keepdims=True)
    grad_resid = grad_result + norm_back(grad_two, resid, rho_two, gain_two)
    grad_attn = grad_resid.astype(BF16)

    grad_attended = dot(w_out, grad_attn, 0, 1).astype(BF16)
    grad_rows = to_rows(grad_attended.reshape(4, q_cols, tok)).reshape(2 * q_cols, row_len)
    grad_q, grad_k, grad_v = attn_bwd(
        length, queries, keys, values, attn_out, grad_rows, lse, hd, 512
    )
    grad_heads = jnp.concatenate(
        [
            grad_q.reshape(2, heads_q, hd, row_len),
            grad_k.reshape(2, heads_k, hd, row_len),
            grad_v.reshape(2, heads_k, hd, row_len),
        ],
        axis=1,
    )
    grad_heads = to_slots(grad_heads).astype(F32)

    def head_back(grad, value, rho, gain):
        turned = turn(grad, -sin_part)
        unit = value * rho
        gain_grad = jnp.sum(turned * unit, axis=(0, 1, 3))
        scaled = turned * gain
        back = rho * (scaled - unit * jnp.mean(scaled * unit, axis=-2, keepdims=True))
        return back.astype(BF16), gain_grad

    back_q, grad_gain_query = head_back(grad_heads[:, :heads_q], raw_q, rho_q, gain_query)
    back_k, grad_gain_key = head_back(
        grad_heads[:, heads_q : heads_q + heads_k], raw_k, rho_k, gain_key
    )
    back = jnp.concatenate(
        [back_q, back_k, grad_heads[:, heads_q + heads_k :].astype(BF16)], axis=1
    ).reshape(4 * proj, tok)
    grad_one = dot(back, w_proj, 0, 1)
    grad_gain_one = jnp.sum(grad_one * x_in * rho_one, axis=0, keepdims=True)
    grad_tokens = grad_resid + norm_back(grad_one, x_in, rho_one, gain_one)
    tokens_grad = spread(grad_tokens.astype(BF16)).astype(F32)

    grad_wproj = dot(normed_one, back, 0, 1).astype(BF16)
    grad_wout = dot(grad_attn, attended, 0, 1).astype(BF16)
    half = width // 2
    attn_parts = []
    for k in range(4):
        part = jnp.concatenate(
            [
                grad_wproj[:, k * proj : (k + 1) * proj],
                grad_wout[:, k * q_cols : (k + 1) * q_cols],
            ],
            axis=1,
        )
        attn_parts.append(plane_reduce(part[:half], part[half:], k in (1, 2)))

    def finish(parts):
        own = z_reduce(parts)
        other = lax.ppermute(own, "ctx", Y_SWAP)
        return jnp.concatenate(
            [jnp.where(ctx == 0, own, other), jnp.where(ctx == 0, other, own)], axis=0
        )

    ffn_grad = finish(ffn_parts)
    attn_grad = finish(attn_parts)

    gain_sums = lax.psum(
        jnp.concatenate(
            [
                restore(grad_gain_one)[0],
                restore(grad_gain_two)[0],
                grad_gain_query,
                grad_gain_key,
            ]
        ),
        ("fsdp", "ctx", "tp"),
    )

    def own_part(at, size):
        return lax.dynamic_slice_in_dim(gain_sums, at + fsdp * (size // 4), size // 4, 0)

    return (
        output,
        teacher_loss,
        tokens_grad,
        own_part(0, width),
        attn_grad[:, :q_cols],
        attn_grad[:, q_cols : q_cols + k_cols],
        attn_grad[:, q_cols + k_cols : proj],
        own_part(2 * width, hd),
        own_part(2 * width + hd, hd),
        attn_grad[:, proj:].T,
        own_part(width, width),
        ffn_grad[:, :units],
        ffn_grad[:, units : 2 * units],
        ffn_grad[:, 2 * units :].T,
    )


def solution(mesh):
    return jax.shard_map(
        per_device_rows if fits(mesh) else per_device_any,
        mesh=mesh,
        in_specs=(
            P("fsdp", "ctx", None),
            P("fsdp", "ctx", None),
            P("fsdp"),
            P("fsdp"),
            P("fsdp", "tp"),
            P("fsdp", "tp"),
            P("fsdp", "tp"),
            P("fsdp"),
            P("fsdp"),
            P("tp", "fsdp"),
            P("fsdp"),
            P("fsdp", "tp"),
            P("fsdp", "tp"),
            P("tp", "fsdp"),
        ),
        out_specs=(
            P("fsdp", "ctx", None),
            P(),
            P("fsdp", "ctx", None),
            P("fsdp"),
            P("fsdp", "tp"),
            P("fsdp", "tp"),
            P("fsdp", "tp"),
            P("fsdp"),
            P("fsdp"),
            P("tp", "fsdp"),
            P("fsdp"),
            P("fsdp", "tp"),
            P("fsdp", "tp"),
            P("tp", "fsdp"),
        ),
        check_vma=False,
    )
```

```python
import functools
import math

import jax
import jax.numpy as jnp
from jax import lax
from jax.experimental import pallas as pl
from jax.experimental.pallas import tpu as pltpu
from jax.sharding import PartitionSpec as P

EPS = 1e-05
THETA = 1000000.0
NEGATIVE = -1e30


def rms_scale(field_in, gain_vec):
    return (
        field_in * lax.rsqrt(jnp.mean(field_in * field_in, axis=-1, keepdims=True) + EPS) * gain_vec
    )


def rotate(field_in, positions):
    half_dim = field_in.shape[-1] // 2
    frequency = THETA ** (-(2.0 * jnp.arange(half_dim, dtype=jnp.float32)) / field_in.shape[-1])
    angles = positions[:, None] * frequency[None, :]
    cos_part = jnp.cos(angles)[:, None, :]
    sin_part = jnp.sin(angles)[:, None, :]
    lower_half = field_in[..., :half_dim]
    upper_half = field_in[..., half_dim:]
    return jnp.concatenate(
        [
            lower_half * cos_part - upper_half * sin_part,
            upper_half * cos_part + lower_half * sin_part,
        ],
        axis=-1,
    )


def linear(left_mat, right_mat):
    return jnp.dot(left_mat, right_mat, preferred_element_type=jnp.float32)


def linear_left(left_mat, right_mat):
    return lax.dot_general(
        left_mat, right_mat, (((0,), (0,)), ((), ())), preferred_element_type=jnp.float32
    )


def linear_right(left_mat, right_mat):
    return lax.dot_general(
        left_mat, right_mat, (((1,), (1,)), ((), ())), preferred_element_type=jnp.float32
    )


def swiglu(gate_act, up_act):
    return jax.nn.silu(gate_act) * up_act


def per_device_any(
    tokens,
    teacher,
    lengths,
    attn_gain,
    q_weight,
    k_weight,
    v_weight,
    q_gain,
    k_gain,
    o_weight,
    ffn_gain,
    gate_weight,
    up_weight,
    down_weight,
):
    (
        gain_one,
        w_query,
        w_key,
        w_value,
        gain_query,
        gain_key,
        w_output,
        gain_two,
        w_gate,
        w_upper,
        w_down,
    ) = (
        lax.all_gather(attn_gain, "fsdp", axis=0, tiled=True),
        lax.all_gather(q_weight, "fsdp", axis=0, tiled=True),
        lax.all_gather(k_weight, "fsdp", axis=0, tiled=True),
        lax.all_gather(v_weight, "fsdp", axis=0, tiled=True),
        lax.all_gather(q_gain, "fsdp", axis=0, tiled=True),
        lax.all_gather(k_gain, "fsdp", axis=0, tiled=True),
        lax.all_gather(o_weight, "fsdp", axis=1, tiled=True),
        lax.all_gather(ffn_gain, "fsdp", axis=0, tiled=True),
        lax.all_gather(gate_weight, "fsdp", axis=0, tiled=True),
        lax.all_gather(up_weight, "fsdp", axis=0, tiled=True),
        lax.all_gather(down_weight, "fsdp", axis=1, tiled=True),
    )
    rows_dev, block_len, model_width = tokens.shape
    count_tok = rows_dev * block_len
    head_dim = gain_query.shape[0]
    q_heads = w_query.shape[1] // head_dim
    kv_heads = w_key.shape[1] // head_dim
    group_size = q_heads // kv_heads
    score_scale = head_dim ** (-0.5)
    row_len = block_len * lax.axis_size("ctx")
    key_block = math.gcd(row_len, 512)
    block_start = lax.axis_index("ctx") * block_len
    tiles_used = (block_start + block_len + key_block - 1) // key_block
    slot_pos = block_start + jnp.arange(block_len, dtype=jnp.int32)
    positions = slot_pos.astype(jnp.float32)
    valid = (slot_pos[None, :] < lengths[:, None]).astype(jnp.float32)
    slots = count_tok * lax.axis_size("fsdp") * lax.axis_size("ctx")
    gain_two_f = gain_two.astype(jnp.float32)
    gain_one_f = gain_one.astype(jnp.float32)
    inputs = tokens.astype(jnp.float32)
    normed_one, back_one = jax.vjp(rms_scale, inputs, gain_one_f)
    normed_low = normed_one.astype(jnp.bfloat16).reshape(count_tok, model_width)
    query_raw = linear(normed_low, w_query)
    key_raw = linear(normed_low, w_key)
    value_raw = linear(normed_low, w_value)

    def heads_post(raw_heads, gain_vec):
        shaped = raw_heads.reshape(rows_dev, block_len, -1, head_dim)
        return rotate(rms_scale(shaped, gain_vec), positions)

    query_rot, query_back = jax.vjp(heads_post, query_raw, gain_query.astype(jnp.float32))
    key_rot, key_back = jax.vjp(heads_post, key_raw, gain_key.astype(jnp.float32))
    queries = query_rot.astype(jnp.bfloat16).reshape(
        rows_dev, block_len, kv_heads, group_size, head_dim
    )
    key_rows = key_rot.astype(jnp.bfloat16).reshape(rows_dev, block_len, kv_heads * head_dim)
    values = value_raw.astype(jnp.bfloat16).reshape(rows_dev, block_len, kv_heads * head_dim)
    keys_all, values_all = (
        lax.all_gather(key_rows, "ctx", axis=1, tiled=True),
        lax.all_gather(values, "ctx", axis=1, tiled=True),
    )

    def key_tile(tile_index):
        tile_start = tile_index * key_block
        key_pos = tile_start + jnp.arange(key_block, dtype=jnp.int32)
        key_part = lax.dynamic_slice_in_dim(keys_all, tile_start, key_block, 1).reshape(
            rows_dev, key_block, kv_heads, head_dim
        )
        value_part = lax.dynamic_slice_in_dim(values_all, tile_start, key_block, 1).reshape(
            rows_dev, key_block, kv_heads, head_dim
        )
        scores = (
            jnp.einsum("rqhgd,rkhd->rhgqk", queries, key_part, preferred_element_type=jnp.float32)
            * score_scale
        )
        allowed = (key_pos[None, None, :] <= slot_pos[None, :, None]) & (
            key_pos[None, None, :] < lengths[:, None, None]
        )
        return (tile_start, scores, allowed[:, None, None], key_part, value_part)

    stat_shape = (rows_dev, kv_heads, group_size, block_len)

    def stats_step(tile_index, carried):
        running_max, running_sum = carried
        tile_start, scores, allowed, key_part, value_part = key_tile(tile_index)
        masked = jnp.where(allowed, scores, NEGATIVE)
        new_max = jnp.maximum(running_max, jnp.max(masked, axis=-1))
        terms = jnp.where(allowed, jnp.exp(masked - new_max[..., None]), 0.0)
        return (new_max, running_sum * jnp.exp(running_max - new_max) + jnp.sum(terms, axis=-1))

    running_max, running_sum = lax.fori_loop(
        0,
        tiles_used,
        stats_step,
        (jnp.full(stat_shape, NEGATIVE, jnp.float32), jnp.zeros(stat_shape, jnp.float32)),
    )
    log_total = running_max + jnp.log(running_sum)
    out_shape = (rows_dev, block_len, kv_heads, group_size, head_dim)

    def value_step(tile_index, carried):
        rounded_out, exact_out = carried
        tile_start, scores, allowed, key_part, value_part = key_tile(tile_index)
        tile_probs = jnp.where(allowed, jnp.exp(scores - log_total[..., None]), 0.0)
        rounded_out = rounded_out + jnp.einsum(
            "rhgqk,rkhd->rqhgd",
            tile_probs.astype(jnp.bfloat16),
            value_part,
            preferred_element_type=jnp.float32,
        )
        exact_out = exact_out + jnp.einsum(
            "rhgqk,rkhd->rqhgd", tile_probs, value_part.astype(jnp.float32)
        )
        return (rounded_out, exact_out)

    rounded_out, exact_out = lax.fori_loop(
        0,
        tiles_used,
        value_step,
        (jnp.zeros(out_shape, jnp.float32), jnp.zeros(out_shape, jnp.float32)),
    )
    attended = rounded_out.astype(jnp.bfloat16).reshape(count_tok, q_heads * head_dim)
    attn_total = lax.psum(linear(attended, w_output), "tp")
    resid = inputs + attn_total.reshape(rows_dev, block_len, model_width)
    normed_two, back_two = jax.vjp(rms_scale, resid, gain_two_f)
    normed_second = normed_two.astype(jnp.bfloat16).reshape(count_tok, model_width)
    gate_act = linear(normed_second, w_gate)
    up_act = linear(normed_second, w_upper)
    hidden_full, back_glu = jax.vjp(swiglu, gate_act, up_act)
    hidden = hidden_full.astype(jnp.bfloat16)
    ffn_total = lax.psum(linear(hidden, w_down), "tp")
    result = resid + ffn_total.reshape(rows_dev, block_len, model_width)
    error_value = result - teacher.astype(jnp.float32)
    valid_col = valid[..., None]
    total_square, total_count = lax.psum(
        (jnp.sum(valid_col * error_value * error_value), jnp.sum(valid)), ("fsdp", "ctx")
    )
    teacher_loss = total_square / (total_count * model_width)
    grad_result = valid_col * error_value * (slots / total_count)
    grad_low = grad_result.astype(jnp.bfloat16).reshape(count_tok, model_width)
    grad_down = linear_left(hidden, grad_low)
    grad_hidden = linear_right(grad_low, w_down)
    grad_gate_full, grad_up_full = back_glu(grad_hidden)
    grad_gate = grad_gate_full.astype(jnp.bfloat16)
    grad_up = grad_up_full.astype(jnp.bfloat16)
    grad_wgate = linear_left(normed_second, grad_gate)
    grad_wup = linear_left(normed_second, grad_up)
    normed_two_part = linear_right(grad_gate, w_gate) + linear_right(grad_up, w_upper)
    grad_normed_two = lax.psum(normed_two_part, "tp")
    grad_resid_norm, grad_gain_two = back_two(
        grad_normed_two.reshape(rows_dev, block_len, model_width)
    )
    grad_resid = grad_result + grad_resid_norm
    grad_attn_low = grad_resid.astype(jnp.bfloat16).reshape(count_tok, model_width)
    grad_woutput = linear_left(attended, grad_attn_low)
    grad_attended = linear_right(grad_attn_low, w_output).astype(jnp.bfloat16).reshape(out_shape)
    delta = jnp.einsum("rqhgd,rqhgd->rhgq", grad_attended.astype(jnp.float32), exact_out)
    full_shape = (rows_dev, row_len, kv_heads * head_dim)

    def grad_step(tile_index, carried):
        grad_queries, grad_keys, grad_values = carried
        tile_start, scores, allowed, key_part, value_part = key_tile(tile_index)
        tile_probs = jnp.where(allowed, jnp.exp(scores - log_total[..., None]), 0.0)
        grad_probs = jnp.einsum(
            "rqhgd,rkhd->rhgqk", grad_attended, value_part, preferred_element_type=jnp.float32
        )
        grad_scores = (tile_probs * (grad_probs - delta[..., None])).astype(jnp.bfloat16)
        grad_queries = (
            grad_queries
            + jnp.einsum(
                "rhgqk,rkhd->rqhgd", grad_scores, key_part, preferred_element_type=jnp.float32
            )
            * score_scale
        )
        key_term = (
            jnp.einsum(
                "rhgqk,rqhgd->rkhd", grad_scores, queries, preferred_element_type=jnp.float32
            )
            * score_scale
        )
        value_term = jnp.einsum(
            "rhgqk,rqhgd->rkhd",
            tile_probs.astype(jnp.bfloat16),
            grad_attended,
            preferred_element_type=jnp.float32,
        )
        grad_keys = lax.dynamic_update_slice_in_dim(
            grad_keys, key_term.reshape(rows_dev, key_block, kv_heads * head_dim), tile_start, 1
        )
        grad_values = lax.dynamic_update_slice_in_dim(
            grad_values, value_term.reshape(rows_dev, key_block, kv_heads * head_dim), tile_start, 1
        )
        return (grad_queries, grad_keys, grad_values)

    grad_queries, grad_keys, grad_values = lax.fori_loop(
        0,
        tiles_used,
        grad_step,
        (
            jnp.zeros(out_shape, jnp.float32),
            jnp.zeros(full_shape, jnp.float32),
            jnp.zeros(full_shape, jnp.float32),
        ),
    )
    key_grad, value_grad = (
        lax.psum_scatter(grad_keys, "ctx", scatter_dimension=1, tiled=True),
        lax.psum_scatter(grad_values, "ctx", scatter_dimension=1, tiled=True),
    )
    grad_query_raw, grad_gain_query = query_back(
        grad_queries.reshape(rows_dev, block_len, q_heads, head_dim)
    )
    grad_key_raw, grad_gain_key = key_back(
        key_grad.reshape(rows_dev, block_len, kv_heads, head_dim)
    )
    query_low = grad_query_raw.astype(jnp.bfloat16)
    key_low = grad_key_raw.astype(jnp.bfloat16)
    value_low = value_grad.reshape(count_tok, kv_heads * head_dim).astype(jnp.bfloat16)
    grad_wquery = linear_left(normed_low, query_low)
    grad_wkey = linear_left(normed_low, key_low)
    grad_wvalue = linear_left(normed_low, value_low)
    normed_part = (
        linear_right(query_low, w_query)
        + linear_right(key_low, w_key)
        + linear_right(value_low, w_value)
    )
    grad_normed_one, grad_gain_query, grad_gain_key = lax.psum(
        (normed_part, grad_gain_query, grad_gain_key), "tp"
    )
    grad_input_norm, grad_gain_one = back_one(
        grad_normed_one.reshape(rows_dev, block_len, model_width)
    )
    tokens_grad = grad_resid + grad_input_norm
    partials = (
        grad_gain_one,
        grad_wquery,
        grad_wkey,
        grad_wvalue,
        grad_gain_query,
        grad_gain_key,
        grad_woutput,
        grad_gain_two,
        grad_wgate,
        grad_wup,
        grad_down,
    )
    pieces = (
        lax.psum_scatter(partials[0], ("fsdp", "ctx"), scatter_dimension=0, tiled=True),
        lax.psum_scatter(partials[1], ("fsdp", "ctx"), scatter_dimension=0, tiled=True),
        lax.psum_scatter(partials[2], ("fsdp", "ctx"), scatter_dimension=0, tiled=True),
        lax.psum_scatter(partials[3], ("fsdp", "ctx"), scatter_dimension=0, tiled=True),
        lax.psum_scatter(partials[4], ("fsdp", "ctx"), scatter_dimension=0, tiled=True),
        lax.psum_scatter(partials[5], ("fsdp", "ctx"), scatter_dimension=0, tiled=True),
        lax.psum_scatter(partials[6], ("fsdp", "ctx"), scatter_dimension=1, tiled=True),
        lax.psum_scatter(partials[7], ("fsdp", "ctx"), scatter_dimension=0, tiled=True),
        lax.psum_scatter(partials[8], ("fsdp", "ctx"), scatter_dimension=0, tiled=True),
        lax.psum_scatter(partials[9], ("fsdp", "ctx"), scatter_dimension=0, tiled=True),
        lax.psum_scatter(partials[10], ("fsdp", "ctx"), scatter_dimension=1, tiled=True),
    )
    summed = (
        lax.all_gather(pieces[0], "ctx", axis=0, tiled=True),
        lax.all_gather(pieces[1], "ctx", axis=0, tiled=True),
        lax.all_gather(pieces[2], "ctx", axis=0, tiled=True),
        lax.all_gather(pieces[3], "ctx", axis=0, tiled=True),
        lax.all_gather(pieces[4], "ctx", axis=0, tiled=True),
        lax.all_gather(pieces[5], "ctx", axis=0, tiled=True),
        lax.all_gather(pieces[6], "ctx", axis=1, tiled=True),
        lax.all_gather(pieces[7], "ctx", axis=0, tiled=True),
        lax.all_gather(pieces[8], "ctx", axis=0, tiled=True),
        lax.all_gather(pieces[9], "ctx", axis=0, tiled=True),
        lax.all_gather(pieces[10], "ctx", axis=1, tiled=True),
    )
    return (
        result.astype(jnp.bfloat16),
        teacher_loss,
        tokens_grad,
        summed[0],
        summed[1],
        summed[2],
        summed[3],
        summed[4],
        summed[5],
        summed[6],
        summed[7],
        summed[8],
        summed[9],
        summed[10],
    )


BF16 = jnp.bfloat16
F32 = jnp.float32
LOG2E = math.log2(math.e)
X_SWAP = [(0, 2), (2, 0), (1, 3), (3, 1)]
CORE_SWAP = [(0, 1), (1, 0), (2, 3), (3, 2)]
Y_SWAP = [(0, 1), (1, 0)]
Z_UP = [(0, 1), (1, 2), (2, 3), (3, 0)]
Z_DOWN = [(0, 3), (1, 0), (2, 1), (3, 2)]
Z_NEAR = [(0, 1), (1, 0), (2, 3), (3, 2)]
Z_FAR = [(0, 2), (2, 0), (1, 3), (3, 1)]
MASKS = (0, 2, 1, 3)
ANY = pl.BlockSpec(memory_space=pl.ANY)
SMEM = pl.BlockSpec(memory_space=pltpu.SMEM)


def fits(mesh):
    return dict(mesh.shape) == {"fsdp": 4, "ctx": 2, "tp": 4}


def dot(left, right, left_dim, right_dim):
    return lax.dot_general(
        left, right, (((left_dim,), (right_dim,)), ((), ())), preferred_element_type=F32
    )


def sigmoid(v):
    return 0.5 * jnp.tanh(0.5 * v) + 0.5


def whole(shape):
    zeros = (0,) * len(shape)
    return pl.BlockSpec(shape, lambda *_: zeros, pipeline_mode=pl.Buffered(1))


def settings(dims, mib):
    return pltpu.CompilerParams(
        dimension_semantics=("arbitrary",) * dims, vmem_limit_bytes=mib << 20
    )


def shape_of(shape, dtype):
    return jax.ShapeDtypeStruct(shape, dtype)


def cost(flops, bytes_accessed):
    return pl.CostEstimate(flops=flops, bytes_accessed=bytes_accessed, transcendentals=0)


def pack_kernel(info, q_ref, k_ref, v_ref, o_ref, g_ref, u_ref, d_ref, attn_ref, ffn_ref):
    ctx = info[2]
    q_cols, k_cols = q_ref.shape[1], k_ref.shape[1]
    attn_ref[:, :q_cols] = q_ref[...]
    attn_ref[:, q_cols : q_cols + k_cols] = k_ref[...]
    attn_ref[:, q_cols + k_cols : q_cols + 2 * k_cols] = v_ref[...]
    attn_ref[:, q_cols + 2 * k_cols :] = o_ref[...].astype(F32).T.astype(BF16)
    third = g_ref.shape[1] // 3
    for j in range(3):
        at = pl.multiple_of(jnp.where(ctx == 0, j, 2 - j) * third, third)
        base = 3 * third * j
        ffn_ref[:, base : base + third] = g_ref[:, pl.ds(at, third)]
        ffn_ref[:, base + third : base + 2 * third] = u_ref[:, pl.ds(at, third)]
        down = d_ref[pl.ds(at, third), :].astype(F32).T.astype(BF16)
        ffn_ref[:, base + 2 * third : base + 3 * third] = down


def pack(info, q, k, v, o, g, u, d):
    rows = q.shape[0]
    attn_cols = q.shape[1] + 2 * k.shape[1] + o.shape[0]
    return pl.pallas_call(
        pack_kernel,
        in_specs=[SMEM] + [pl.BlockSpec(memory_space=pltpu.VMEM)] * 7,
        out_specs=[pl.BlockSpec(memory_space=pltpu.VMEM)] * 2,
        out_shape=[shape_of((rows, attn_cols), BF16), shape_of((rows, 3 * g.shape[1]), BF16)],
        compiler_params=pltpu.CompilerParams(vmem_limit_bytes=24 << 20),
        cost_estimate=cost(0, 6 << 20),
        name="pack",
    )(info, q, k, v, o, g, u, d)


def norm_one_kernel(info, tok_ref, gain_ref, x_ref, nt_ref, x32):
    quarter = x_ref.shape[1] // 4
    for p, mask in enumerate(MASKS):
        at = pl.multiple_of(jnp.bitwise_xor(info[1], mask) * quarter, quarter)
        part = tok_ref[0, :, pl.ds(at, quarter)]
        x_ref[:, p * quarter : (p + 1) * quarter] = part
        x32[:, p * quarter : (p + 1) * quarter] = part.astype(F32)
    x = x32[...]
    rho = lax.rsqrt(jnp.mean(x * x, axis=-1, keepdims=True) + EPS)
    nt_ref[...] = (x * rho * gain_ref[...]).T.astype(BF16)


def norm_one(info, tokens, gain, tile):
    _, tok, width = tokens.shape
    return pl.pallas_call(
        norm_one_kernel,
        grid_spec=pltpu.PrefetchScalarGridSpec(
            num_scalar_prefetch=1,
            grid=(tok // tile,),
            in_specs=[
                pl.BlockSpec((1, tile, width), lambda i, info: (info[0], i, 0)),
                pl.BlockSpec((1, width), lambda i, info: (0, 0)),
            ],
            out_specs=[
                pl.BlockSpec((tile, width), lambda i, info: (i, 0)),
                pl.BlockSpec((width, tile), lambda i, info: (0, i)),
            ],
            scratch_shapes=[pltpu.VMEM((tile, width), F32)],
        ),
        out_shape=[shape_of((tok, width), BF16), shape_of((width, tok), BF16)],
        compiler_params=settings(1, 24),
        cost_estimate=cost(0, 6 << 20),
        name="norm_one",
    )(info, tokens, gain)


def proj_kernel(heads, info, w_ref, nt_ref, cos_ref, sin_ref, qg_ref, kg_ref, rot_ref, raw_ref):
    hd = qg_ref.shape[0]
    tok = nt_ref.shape[1]
    half = hd // 2
    raw = dot(w_ref[0], nt_ref[...], 0, 0)
    cos_part, sin_part = cos_ref[...], sin_ref[...]
    heads_q, heads_k = heads
    raw_ref[...] = raw.astype(BF16)
    for h in range(heads_q + heads_k):
        v = raw[h * hd : (h + 1) * hd]
        rho = lax.rsqrt(jnp.mean(v * v, axis=0, keepdims=True) + EPS)
        v = v * rho * (qg_ref[...] if h < heads_q else kg_ref[...])
        a, b = v[:half], v[half:]
        rot_ref[h * hd : h * hd + half, :] = (a * cos_part - b * sin_part).astype(BF16)
        rot_ref[h * hd + half : (h + 1) * hd, :] = (b * cos_part + a * sin_part).astype(BF16)
    at = (heads_q + heads_k) * hd
    rot_ref[at:, :] = raw[at:].astype(BF16)


def project(info, w_proj, normed_t, cos_part, sin_part, gain_q, gain_k, heads, block):
    _, width, cols = w_proj.shape
    tok = normed_t.shape[1]
    tile = min(512, tok)
    const = lambda a: pl.BlockSpec(a.shape, lambda i, info: (0, 0))
    tab = lambda a: pl.BlockSpec((a.shape[0], tile), lambda i, info: (0, i))
    return pl.pallas_call(
        functools.partial(proj_kernel, heads),
        grid_spec=pltpu.PrefetchScalarGridSpec(
            num_scalar_prefetch=1,
            grid=(tok // tile,),
            in_specs=[
                pl.BlockSpec((1, width, cols), lambda i, info: (block(info), 0, 0)),
                tab(normed_t),
                tab(cos_part),
                tab(sin_part),
                const(gain_q),
                const(gain_k),
            ],
            out_specs=[pl.BlockSpec((cols, tile), lambda i, info: (0, i))] * 2,
        ),
        out_shape=[shape_of((cols, tok), BF16), shape_of((cols, tok), BF16)],
        compiler_params=settings(1, 24),
        cost_estimate=cost(2 * width * cols * tok, 6 << 20),
        name="project",
    )(info, w_proj, normed_t, cos_part, sin_part, gain_q, gain_k)


def head_back_kernel(
    heads, info, dm_ref, dt_ref, rm_ref, rt_ref, cos_ref, sin_ref, qg_ref, kg_ref, out_ref, gg_ref
):
    step, part = pl.program_id(0), pl.program_id(1)
    hd = qg_ref.shape[0]
    half = hd // 2
    heads_q, heads_k = heads
    cos_part, sin_part = cos_ref[...], sin_ref[...]
    tile = cos_part.shape[1]

    @pl.when((step == 0) & (part == 0))
    def _():
        gg_ref[...] = jnp.zeros_like(gg_ref)

    def work(d_ref, r_ref):
        gain_q = jnp.zeros((hd, 1), F32)
        gain_k = jnp.zeros((hd, 1), F32)
        done = []
        for h in range(heads_q + heads_k):
            is_q = h < heads_q
            g = d_ref[h * hd : (h + 1) * hd, :].astype(F32)
            raw = r_ref[h * hd : (h + 1) * hd, :].astype(F32)
            a, b = g[:half], g[half:]
            turned = jnp.concatenate(
                [a * cos_part + b * sin_part, b * cos_part - a * sin_part], axis=0
            )
            rho = lax.rsqrt(jnp.mean(raw * raw, axis=0, keepdims=True) + EPS)
            unit = raw * rho
            prod = turned * unit
            scaled = turned * (qg_ref[...] if is_q else kg_ref[...])
            mean = jnp.mean(scaled * unit, axis=0, keepdims=True)
            done.append(rho * (scaled - unit * mean))
            total = jnp.sum(prod, axis=1, keepdims=True)
            if is_q:
                gain_q = gain_q + total
            else:
                gain_k = gain_k + total
        done.append(d_ref[(heads_q + heads_k) * hd :, :].astype(F32))
        out_ref[0] = jnp.concatenate(done, axis=0).T.astype(BF16)
        lane = lax.broadcasted_iota(jnp.int32, gg_ref.shape, 1)
        gg_ref[...] += jnp.where(lane == 0, gain_q, jnp.where(lane == 1, gain_k, 0.0))

    @pl.when(step == 0)
    def _():
        work(dm_ref, rm_ref)

    @pl.when(step == 1)
    def _():
        work(dt_ref, rt_ref)


def head_back(info, grad_mine, grad_theirs, raw_mine, raw_theirs, cos_part, sin_part, gq, gk, heads):
    cols, tok = grad_mine.shape
    tile = min(512, tok)
    mine = pl.BlockSpec((cols, tile), lambda s, i, info: (0, jnp.where(s == 0, i, tok // tile - 1)))
    theirs = pl.BlockSpec((cols, tile), lambda s, i, info: (0, jnp.where(s == 0, 0, i)))
    tab = lambda a: pl.BlockSpec((a.shape[0], tile), lambda s, i, info: (0, i))
    const = lambda a: pl.BlockSpec(a.shape, lambda s, i, info: (0, 0))
    return pl.pallas_call(
        functools.partial(head_back_kernel, heads),
        grid_spec=pltpu.PrefetchScalarGridSpec(
            num_scalar_prefetch=1,
            grid=(2, tok // tile),
            in_specs=[
                mine,
                theirs,
                mine,
                theirs,
                tab(cos_part),
                tab(sin_part),
                const(gq),
                const(gk),
            ],
            out_specs=[
                pl.BlockSpec(
                    (1, tile, cols), lambda s, i, info: (jnp.bitwise_xor(info[2], s), i, 0)
                ),
                pl.BlockSpec((gq.shape[0], 128), lambda s, i, info: (0, 0)),
            ],
        ),
        out_shape=[shape_of((2, tok, cols), BF16), shape_of((gq.shape[0], 128), F32)],
        compiler_params=settings(2, 24),
        cost_estimate=cost(0, 8 << 20),
        name="head_back",
    )(info, grad_mine, grad_theirs, raw_mine, raw_theirs, cos_part, sin_part, gq, gk)


def load_rows(info, mine_ref, got_ref, rows, sems):
    tok = mine_ref.shape[1]
    ctx = info[2]
    here = pl.multiple_of(ctx * tok, tok)
    there = pl.multiple_of((1 - ctx) * tok, tok)
    one = pltpu.make_async_copy(mine_ref, rows.at[:, pl.ds(here, tok)], sems.at[0])
    two = pltpu.make_async_copy(got_ref, rows.at[:, pl.ds(there, tok)], sems.at[1])
    one.start()
    two.start()
    one.wait()
    two.wait()


def keys_with_bias(keys, length):
    hd, slots = keys.shape
    pos = lax.broadcasted_iota(jnp.int32, (hd, slots), 1)
    row = lax.broadcasted_iota(jnp.int32, (hd, slots), 0)
    bias = jnp.where((row == 0) & (pos >= length), NEGATIVE, 0.0)
    return jnp.concatenate([keys.astype(F32), bias], axis=0).T.astype(BF16)


def query_with_one(pair):
    one_row = jnp.where(lax.broadcasted_iota(jnp.int32, pair.shape, 0) == 0, 1.0, 0.0)
    return jnp.concatenate([pair, one_row.astype(BF16)], axis=0)


def causal(scores, width):
    key_pos = lax.broadcasted_iota(jnp.int32, (width, width), 0)
    query_pos = lax.broadcasted_iota(jnp.int32, (width, width), 1)
    allowed = key_pos <= query_pos
    return jnp.where(jnp.concatenate([allowed, allowed], axis=1), scores, NEGATIVE)


def attn_fwd_kernel(
    width, hd, info, mine_ref, got_ref, keep_ref, send_ref, lse_ref, rows, key_rows, sems
):
    head, block = pl.program_id(0), pl.program_id(1)
    heads_k = pl.num_programs(0)
    scale = hd**-0.5 * LOG2E
    length = info[3]
    key_at = pl.multiple_of(heads_k * 2 * hd + head * hd, hd)
    value_at = pl.multiple_of(heads_k * 3 * hd + head * hd, hd)
    query_at = pl.multiple_of(head * 2 * hd, 2 * hd)

    @pl.when((head == 0) & (block == 0))
    def _():
        load_rows(info, mine_ref, got_ref, rows, sems)

    @pl.when(block == 0)
    def _():
        key_rows[...] = keys_with_bias(rows[pl.ds(key_at, hd), :], length)

    start = pl.multiple_of(block * width, width)
    both = rows[pl.ds(query_at, 2 * hd), pl.ds(start, width)]
    query = query_with_one(jnp.concatenate([both[:hd], both[hd:]], axis=1))

    def tile(at, carried, diagonal):
        out, total = carried
        scores = dot(key_rows[pl.ds(at, width), :], query, 1, 0)
        if diagonal:
            scores = causal(scores, width)
        probs = jnp.exp2(scores * scale)
        total = total + jnp.sum(probs, axis=0, keepdims=True)
        out = out + dot(rows[pl.ds(value_at, hd), pl.ds(at, width)], probs.astype(BF16), 1, 0)
        return out, total

    carried = (jnp.zeros((hd, 2 * width), F32), jnp.zeros((1, 2 * width), F32))
    full = jnp.minimum(block, lax.div(length + width - 1, width))
    carried = lax.fori_loop(
        0, full, lambda j, c: tile(pl.multiple_of(j * width, width), c, False), carried
    )
    out, total = tile(start, carried, True)
    out = out * (1.0 / total)
    out = jnp.concatenate([out[:, :width], out[:, width:]], axis=0).T.astype(BF16)
    here = block // 2 == info[2]

    @pl.when(here)
    def _():
        keep_ref[...] = out

    @pl.when(jnp.logical_not(here))
    def _():
        send_ref[...] = out

    log_total = jnp.log2(total)
    lse_ref[0, 0:1, :] = log_total[:, :width]
    lse_ref[0, 1:2, :] = log_total[:, width:]


def keep_block(i, info):
    return jnp.clip(i - 2 * info[2], 0, 1)


def send_block(i, info):
    return jnp.clip(i - 2 * (1 - info[2]), 0, 1)


def attn_fwd(info, mine, got, hd):
    cols, tok = mine.shape
    heads_k = cols // (4 * hd)
    width = tok // 2
    return pl.pallas_call(
        functools.partial(attn_fwd_kernel, width, hd),
        grid_spec=pltpu.PrefetchScalarGridSpec(
            num_scalar_prefetch=1,
            grid=(heads_k, 4),
            in_specs=[ANY, ANY],
            out_specs=[
                pl.BlockSpec((width, 2 * hd), lambda h, i, info: (keep_block(i, info), h)),
                pl.BlockSpec((width, 2 * hd), lambda h, i, info: (send_block(i, info), h)),
                pl.BlockSpec((1, 2, width), lambda h, i, info: (h, 0, i)),
            ],
            scratch_shapes=[
                pltpu.VMEM((cols, 2 * tok), BF16),
                pltpu.VMEM((2 * tok, 2 * hd), BF16),
                pltpu.SemaphoreType.DMA((2,)),
            ],
        ),
        out_shape=[
            shape_of((tok, heads_k * 2 * hd), BF16),
            shape_of((tok, heads_k * 2 * hd), BF16),
            shape_of((heads_k, 2, 2 * tok), F32),
        ],
        compiler_params=settings(2, 32),
        cost_estimate=cost(heads_k * 2 * tok * 2 * tok * 256 * 4, 8 << 20),
        name="attn_fwd",
    )(info, mine, got)


def attn_bwd_kernel(
    width,
    hd,
    info,
    mine_ref,
    got_ref,
    ok_ref,
    os_ref,
    gk_ref,
    gs_ref,
    lse_ref,
    keep_ref,
    send_ref,
    rows,
    key_rows,
    value_rows,
    key_sum,
    value_sum,
    sems,
):
    head, block = pl.program_id(0), pl.program_id(1)
    heads_k = pl.num_programs(0)
    scale = hd**-0.5
    length = info[3]
    ctx = info[2]
    tok = keep_ref.shape[1]
    key_at = pl.multiple_of(heads_k * 2 * hd + head * hd, hd)
    value_at = pl.multiple_of(heads_k * 3 * hd + head * hd, hd)
    query_at = pl.multiple_of(head * 2 * hd, 2 * hd)

    @pl.when((head == 0) & (block == 0))
    def _():
        load_rows(info, mine_ref, got_ref, rows, sems)

    @pl.when(block == 0)
    def _():
        key_rows[...] = keys_with_bias(rows[pl.ds(key_at, hd), :], length)
        value_rows[...] = rows[pl.ds(value_at, hd), :].astype(F32).T.astype(BF16)
        key_sum[...] = jnp.zeros_like(key_sum)
        value_sum[...] = jnp.zeros_like(value_sum)

    start = pl.multiple_of(block * width, width)
    here = block // 2 == ctx

    def store_query(value):
        at = pl.ds(pl.multiple_of((block % 2) * width, width), width)

        @pl.when(here)
        def _():
            keep_ref[pl.ds(query_at, 2 * hd), at] = value

        @pl.when(jnp.logical_not(here))
        def _():
            send_ref[pl.ds(query_at, 2 * hd), at] = value

    @pl.when(block * width < length)
    def _():
        both = rows[pl.ds(query_at, 2 * hd), pl.ds(start, width)]
        pair = jnp.concatenate([both[:hd], both[hd:]], axis=1)
        query = query_with_one(pair)
        query_rows = pair.astype(F32).T.astype(BF16)
        grad_wide = jnp.where(here, gk_ref[...].astype(F32), gs_ref[...].astype(F32))
        out_wide = jnp.where(here, ok_ref[...].astype(F32), os_ref[...].astype(F32))
        grad_rows = jnp.concatenate([grad_wide[:, :hd], grad_wide[:, hd:]], axis=0).astype(BF16)
        grad_t = grad_wide.T
        prod = (grad_wide * out_wide).T
        grad = jnp.concatenate([grad_t[:hd], grad_t[hd:]], axis=1).astype(BF16)
        delta = jnp.concatenate(
            [
                jnp.sum(prod[:hd], axis=0, keepdims=True),
                jnp.sum(prod[hd:], axis=0, keepdims=True),
            ],
            axis=1,
        )
        lse = jnp.concatenate([lse_ref[0, 0:1, :], lse_ref[0, 1:2, :]], axis=1)

        def tile(at, query_sum, diagonal):
            scores = dot(key_rows[pl.ds(at, width), :], query, 1, 0)
            if diagonal:
                scores = causal(scores, width)
            probs = jnp.exp2(scores * (scale * LOG2E) - lse)
            grad_probs = dot(value_rows[pl.ds(at, width), :], grad, 1, 0)
            grad_scores = (probs * (grad_probs - delta)).astype(BF16)
            value_sum[pl.ds(at, width), :] += dot(probs.astype(BF16), grad_rows, 1, 0)
            key_sum[pl.ds(at, width), :] += dot(grad_scores, query_rows, 1, 0)
            return query_sum + dot(rows[pl.ds(key_at, hd), pl.ds(at, width)], grad_scores, 1, 0)

        query_sum = lax.fori_loop(
            0,
            block,
            lambda j, s: tile(pl.multiple_of(j * width, width), s, False),
            jnp.zeros((hd, 2 * width), F32),
        )
        query_sum = tile(start, query_sum, True) * scale
        store_query(
            jnp.concatenate([query_sum[:, :width], query_sum[:, width:]], axis=0).astype(BF16)
        )

    @pl.when(block * width >= length)
    def _():
        store_query(jnp.zeros((2 * hd, width), BF16))

    @pl.when(block == 3)
    def _():
        for at, total in ((key_at, key_sum[...] * scale), (value_at, value_sum[...])):
            total = total.T.astype(BF16)
            left, right = total[:, :tok], total[:, tok:]

            @pl.when(ctx == 0)
            def _():
                keep_ref[pl.ds(at, hd), :] = left
                send_ref[pl.ds(at, hd), :] = right

            @pl.when(ctx == 1)
            def _():
                keep_ref[pl.ds(at, hd), :] = right
                send_ref[pl.ds(at, hd), :] = left


def attn_bwd(info, mine, got, out_keep, out_send, grad_keep, grad_send, lse, hd):
    cols, tok = mine.shape
    heads_k = cols // (4 * hd)
    width = tok // 2
    keep = pl.BlockSpec((width, 2 * hd), lambda h, i, info: (keep_block(i, info), h))
    send = pl.BlockSpec((width, 2 * hd), lambda h, i, info: (send_block(i, info), h))
    full = pl.BlockSpec((cols, tok), lambda h, i, info: (0, 0))
    return pl.pallas_call(
        functools.partial(attn_bwd_kernel, width, hd),
        grid_spec=pltpu.PrefetchScalarGridSpec(
            num_scalar_prefetch=1,
            grid=(heads_k, 4),
            in_specs=[
                ANY,
                ANY,
                keep,
                send,
                keep,
                send,
                pl.BlockSpec((1, 2, width), lambda h, i, info: (h, 0, i)),
            ],
            out_specs=[full, full],
            scratch_shapes=[
                pltpu.VMEM((cols, 2 * tok), BF16),
                pltpu.VMEM((2 * tok, 2 * hd), BF16),
                pltpu.VMEM((2 * tok, hd), BF16),
                pltpu.VMEM((2 * tok, hd), F32),
                pltpu.VMEM((2 * tok, hd), F32),
                pltpu.SemaphoreType.DMA((2,)),
            ],
        ),
        out_shape=[shape_of((cols, tok), BF16), shape_of((cols, tok), BF16)],
        compiler_params=settings(2, 40),
        cost_estimate=cost(heads_k * 5 * tok * 2 * tok * 256 * 4, 12 << 20),
        name="attn_bwd",
    )(info, mine, got, out_keep, out_send, grad_keep, grad_send, lse)


def out_proj_kernel(info, x_ref, a0, a1, b0, b1, w_ref, gain_ref, r_ref, n_ref, nt_ref, att_ref):
    ctx = info[2]
    total = x_ref[...].astype(F32)
    for j, ref, side in ((0, a0, ctx), (1, a1, ctx), (0, b0, 1 - ctx), (1, b1, 1 - ctx)):
        block = 2 * side + j
        part = ref[...]
        att_ref[block] = part
        total = total + dot(part, w_ref[block], 1, 1)
    rho = lax.rsqrt(jnp.mean(total * total, axis=-1, keepdims=True) + EPS)
    normed = total * rho * gain_ref[...]
    r_ref[...] = total
    n_ref[...] = normed.astype(BF16)
    nt_ref[...] = normed.T.astype(BF16)


def out_proj(info, x, mine, theirs, w_out, gain, tile):
    tok, width = x.shape
    feats = w_out.shape[2]
    rows_of = lambda n: pl.BlockSpec((tile, n), lambda i, info: (i, 0))
    return pl.pallas_call(
        out_proj_kernel,
        grid_spec=pltpu.PrefetchScalarGridSpec(
            num_scalar_prefetch=1,
            grid=(tok // tile,),
            in_specs=[rows_of(width)]
            + [rows_of(feats)] * 4
            + [whole(w_out.shape), pl.BlockSpec((1, width), lambda i, info: (0, 0))],
            out_specs=[
                rows_of(width),
                rows_of(width),
                pl.BlockSpec((width, tile), lambda i, info: (0, i)),
                pl.BlockSpec((4, tile, feats), lambda i, info: (0, i, 0)),
            ],
        ),
        out_shape=[
            shape_of((tok, width), F32),
            shape_of((tok, width), BF16),
            shape_of((width, tok), BF16),
            shape_of((4, tok, feats), BF16),
        ],
        compiler_params=settings(1, 32),
        cost_estimate=cost(2 * tok * width * 4 * feats, 16 << 20),
        name="out_proj",
    )(info, x, *mine, *theirs, w_out, gain)


def norm_two_back_kernel(
    info, g_ref, r_ref, gr_ref, gain_ref, w_ref, gres_ref, gat_ref, a0, a1, b0, b1, gg_ref
):
    ctx = info[2]
    grad, resid = g_ref[...], r_ref[...]
    rho = lax.rsqrt(jnp.mean(resid * resid, axis=-1, keepdims=True) + EPS)
    unit = resid * rho
    scaled = grad * gain_ref[...]
    back = rho * (scaled - unit * jnp.mean(scaled * unit, axis=-1, keepdims=True))
    total = gr_ref[...] + back
    gres_ref[...] = total
    low = total.astype(BF16)
    gat_ref[...] = total.T.astype(BF16)

    @pl.when(pl.program_id(0) == 0)
    def _():
        gg_ref[...] = jnp.zeros_like(gg_ref)

    gg_ref[...] += jnp.sum(grad * unit, axis=0, keepdims=True)
    for j, ref, side in ((0, a0, ctx), (1, a1, ctx), (0, b0, 1 - ctx), (1, b1, 1 - ctx)):
        ref[...] = dot(low, w_ref[2 * side + j], 1, 0).astype(BF16)


def norm_two_back(info, grad, resid, grad_result, gain, w_out, tile):
    tok, width = grad.shape
    feats = w_out.shape[2]
    rows_of = lambda n: pl.BlockSpec((tile, n), lambda i, info: (i, 0))
    row = pl.BlockSpec((1, width), lambda i, info: (0, 0))
    return pl.pallas_call(
        norm_two_back_kernel,
        grid_spec=pltpu.PrefetchScalarGridSpec(
            num_scalar_prefetch=1,
            grid=(tok // tile,),
            in_specs=[rows_of(width)] * 3 + [row, whole(w_out.shape)],
            out_specs=[rows_of(width), pl.BlockSpec((width, tile), lambda i, info: (0, i))]
            + [rows_of(feats)] * 4
            + [row],
        ),
        out_shape=[shape_of((tok, width), F32), shape_of((width, tok), BF16)]
        + [shape_of((tok, feats), BF16)] * 4
        + [shape_of((1, width), F32)],
        compiler_params=settings(1, 32),
        cost_estimate=cost(2 * tok * width * 4 * feats, 24 << 20),
        name="norm_two_back",
    )(info, grad, resid, grad_result, gain, w_out)


def norm_one_back_kernel(info, p0, p1, w_ref, x_ref, gres_ref, gain_ref, out_ref, gg_ref):
    quarter = x_ref.shape[1] // 4
    grad = dot(p0[0], w_ref[0], 1, 1)
    grad = grad + dot(p1[0], w_ref[1], 1, 1)
    grad = grad + dot(p0[1], w_ref[2], 1, 1)
    grad = grad + dot(p1[1], w_ref[3], 1, 1)
    x = x_ref[...].astype(F32)
    rho = lax.rsqrt(jnp.mean(x * x, axis=-1, keepdims=True) + EPS)
    unit = x * rho
    scaled = grad * gain_ref[...]
    back = rho * (scaled - unit * jnp.mean(scaled * unit, axis=-1, keepdims=True))
    total = (gres_ref[...] + back).astype(BF16)
    for p, mask in enumerate(MASKS):
        at = pl.multiple_of(jnp.bitwise_xor(info[1], mask) * quarter, quarter)
        out_ref[:, pl.ds(at, quarter)] = total[:, p * quarter : (p + 1) * quarter]

    @pl.when(pl.program_id(0) == 0)
    def _():
        gg_ref[...] = jnp.zeros_like(gg_ref)

    gg_ref[...] += jnp.sum(grad * unit, axis=0, keepdims=True)


def norm_one_back(info, pairs, w_proj, x, grad_resid, gain, tile):
    tok, width = x.shape
    cols = w_proj.shape[2]
    rows_of = lambda n: pl.BlockSpec((tile, n), lambda i, info: (i, 0))
    pair = pl.BlockSpec((2, tile, cols), lambda i, info: (0, i, 0))
    row = pl.BlockSpec((1, width), lambda i, info: (0, 0))
    return pl.pallas_call(
        norm_one_back_kernel,
        grid_spec=pltpu.PrefetchScalarGridSpec(
            num_scalar_prefetch=1,
            grid=(tok // tile,),
            in_specs=[pair, pair, whole(w_proj.shape), rows_of(width), rows_of(width), row],
            out_specs=[rows_of(width), row],
        ),
        out_shape=[shape_of((tok, width), BF16), shape_of((1, width), F32)],
        compiler_params=settings(1, 32),
        cost_estimate=cost(2 * tok * width * 4 * cols, 18 << 20),
        name="norm_one_back",
    )(info, *pairs, w_proj, x, grad_resid, gain)


def weight_copies(pieces, gate_up, down, gate_up_sem, down_sem):
    own, far, last, own2, far2, last2 = pieces
    rows, cols = own.shape
    chunk = cols // 3
    third = chunk // 3
    wide, thin = [], []
    for p, (ref, first) in enumerate(((own, 0), (far, 0), (own2, 0), (far2, 0))):
        for j in range(3):
            src = ref
            at = j * chunk
            if p % 2 == 1 and j == 2:
                src, at = (last, last2)[p // 2], 0
            block = pl.ds(p * rows, rows)
            wide.append(
                pltpu.make_async_copy(
                    src.at[:, pl.ds(at, 2 * third)],
                    gate_up.at[block, pl.ds(j * 2 * third, 2 * third)],
                    gate_up_sem,
                )
            )
            thin.append(
                pltpu.make_async_copy(
                    src.at[:, pl.ds(at + 2 * third, third)],
                    down.at[block, pl.ds(j * third, third)],
                    down_sem,
                )
            )
    return wide, thin


def split_act(act):
    third = act.shape[1] // 6
    part = lambda j: act[:, j * third : (j + 1) * third]
    return [(part(0), part(1)), (part(2), part(3)), (part(4), part(5))]


def ffn_fwd_kernel(
    tile,
    info,
    scale,
    x_ref,
    resid_ref,
    teach_ref,
    *rest,
):
    pieces = [rest[6 * s : 6 * s + 6] for s in range(4)]
    act_ref, hid_ref, out_ref, gres_ref, low_ref, lowt_ref, sq_ref = rest[24:31]
    gate_up, down, total, sems = rest[31:]
    step, part = pl.program_id(0), pl.program_id(1)
    width = x_ref.shape[1]
    quarter = width // 4
    third = down.shape[2] // 3

    def copies(s):
        return weight_copies(pieces[s], gate_up.at[s], down.at[s], sems.at[s, 0], sems.at[s, 1])

    @pl.when((step == 0) & (part == 0))
    def _():
        for s in range(4):
            wide, thin = copies(s)
            for copy in wide + thin:
                copy.start()

    for s in range(4):

        @pl.when((step == s) & (part == 0))
        def _():
            pltpu.make_async_copy(gate_up.at[s], gate_up.at[s], sems.at[s, 0]).wait()
            pltpu.make_async_copy(down.at[s], down.at[s], sems.at[s, 1]).wait()

    rows = pl.ds(pl.multiple_of(part * tile, tile), tile)
    act = dot(x_ref[rows, :], gate_up[step], 1, 0)
    for j, (gate, upper) in enumerate(split_act(act)):
        hid_ref[0, :, j * third : (j + 1) * third] = (gate * sigmoid(gate) * upper).astype(BF16)
    act_ref[0] = act.astype(BF16)
    grown = dot(hid_ref[0], down[step], 1, 1)

    @pl.when(step == 0)
    def _():
        total[rows, :] = resid_ref[rows, :] + grown

    @pl.when((step > 0) & (step < 3))
    def _():
        total[rows, :] += grown

    @pl.when(step == 3)
    def _():
        result = total[rows, :] + grown
        total[rows, :] = result
        tok = x_ref.shape[0]
        slot = info[2] * tok + part * tile + lax.broadcasted_iota(jnp.int32, (tile, 1), 0)
        valid = jnp.where(slot < info[3], 1.0, 0.0)
        square = jnp.zeros((tile, quarter), F32)
        for p, mask in enumerate(MASKS):
            at = pl.multiple_of(jnp.bitwise_xor(info[1], mask) * quarter, quarter)
            cols = slice(p * quarter, (p + 1) * quarter)
            value = result[:, cols]
            out_ref[:, pl.ds(at, quarter)] = value.astype(BF16)
            error = valid * (value - teach_ref[0, :, pl.ds(at, quarter)].astype(F32))
            square = square + error * error
            grad = error * scale[0]
            gres_ref[:, cols] = grad
            low_ref[:, cols] = grad.astype(BF16)
            lowt_ref[cols, :] = grad.T.astype(BF16)

        @pl.when(part == 0)
        def _():
            sq_ref[...] = jnp.zeros_like(sq_ref)

        sq_ref[...] += jnp.sum(square, axis=0, keepdims=True)


def ffn_fwd(info, scale, x, resid, teacher, pieces, tile):
    tok, width = x.shape
    units = pieces[0][0].shape[1] // 3
    last = lambda s, i: jnp.where(s == 3, i, 0)
    tiles = lambda n: pl.BlockSpec((tile, n), lambda s, i, info: (last(s, i), 0))
    return pl.pallas_call(
        functools.partial(ffn_fwd_kernel, tile),
        grid_spec=pltpu.PrefetchScalarGridSpec(
            num_scalar_prefetch=1,
            grid=(4, tok // tile),
            in_specs=[
                SMEM,
                whole((tok, width)),
                whole((tok, width)),
                pl.BlockSpec((1, tile, width), lambda s, i, info: (info[0], last(s, i), 0)),
            ]
            + [ANY] * 24,
            out_specs=[
                pl.BlockSpec((1, tile, 2 * units), lambda s, i, info: (s, i, 0)),
                pl.BlockSpec((1, tile, units), lambda s, i, info: (s, i, 0)),
                tiles(width),
                tiles(width),
                tiles(width),
                pl.BlockSpec((width, tile), lambda s, i, info: (0, last(s, i))),
                pl.BlockSpec((1, width // 4), lambda s, i, info: (0, 0)),
            ],
            scratch_shapes=[
                pltpu.VMEM((4, width, 2 * units), BF16),
                pltpu.VMEM((4, width, units), BF16),
                pltpu.VMEM((tok, width), F32),
                pltpu.SemaphoreType.DMA((4, 2)),
            ],
        ),
        out_shape=[
            shape_of((4, tok, 2 * units), BF16),
            shape_of((4, tok, units), BF16),
            shape_of((tok, width), BF16),
            shape_of((tok, width), F32),
            shape_of((tok, width), BF16),
            shape_of((width, tok), BF16),
            shape_of((1, width // 4), F32),
        ],
        compiler_params=settings(2, 61),
        cost_estimate=cost(2 * tok * width * units * 12, 70 << 20),
        name="ffn_fwd",
    )(info, scale, x, resid, teacher, *[ref for group in pieces for ref in group])


def ffn_bwd_kernel(steps, first, low_ref, act_ref, hid_ref, xt_ref, lowt_ref, *rest):
    pieces = rest[:6]
    rest = rest[6:]
    if not first:
        in_ref, rest = rest[0], rest[1:]
    out_ref, keep_ref, send_ref, gate_up, down, dact_all, hid_all, sems = rest
    step = pl.program_id(0)
    units = down.shape[1]
    third = units // 3
    tile = low_ref.shape[0]

    @pl.when(step == 0)
    def _():
        wide, thin = weight_copies(pieces, gate_up, down, sems.at[0], sems.at[1])
        for copy in thin + wide:
            copy.start()
        pltpu.make_async_copy(down, down, sems.at[1]).wait()

    @pl.when(step < steps)
    def _():
        rows = pl.ds(pl.multiple_of(step * tile, tile), tile)
        grad_hidden = dot(low_ref[...], down[...], 1, 0)
        for j, (gate, upper) in enumerate(split_act(act_ref[0])):
            grad = grad_hidden[:, j * third : (j + 1) * third]
            gate, upper = gate.astype(F32), upper.astype(F32)
            sig = sigmoid(gate)
            silu = gate * sig
            at = 2 * j * third
            dact_all[rows, at : at + third] = (
                grad * upper * (sig + silu - silu * sig)
            ).astype(BF16)
            dact_all[rows, at + third : at + 2 * third] = (grad * silu).astype(BF16)
        hid_all[rows, :] = hid_ref[0]

        @pl.when(step == 0)
        def _():
            pltpu.make_async_copy(gate_up, gate_up, sems.at[0]).wait()

        grown = dot(dact_all[rows, :], gate_up[...], 1, 1)
        out_ref[...] = grown if first else in_ref[...] + grown

    def weight_rows(target):
        target[:, : 2 * units] = dot(xt_ref[...], dact_all[...], 1, 0).astype(BF16)
        target[:, 2 * units :] = dot(lowt_ref[...], hid_all[...], 1, 0).astype(BF16)

    @pl.when((step >= steps) & (step < steps + 2))
    def _():
        weight_rows(send_ref)

    @pl.when(step >= steps + 2)
    def _():
        weight_rows(keep_ref)


def ffn_bwd(block, low, acts, hiddens, pieces, total, xt, lowt, tile):
    tok, width = low.shape
    units = hiddens.shape[2]
    steps = tok // tile
    quarter = width // 4
    first = total is None
    clip = lambda i: jnp.minimum(i, steps - 1)
    rows_of = lambda n: pl.BlockSpec((tile, n), lambda i: (clip(i), 0))
    slab = lambda n: pl.BlockSpec((1, tile, n), lambda i: (block, clip(i), 0))
    feature = lambda i: (jnp.where(i < steps + 2, jnp.maximum(i - steps, 0) + 2, i - steps - 2), 0)
    return pl.pallas_call(
        functools.partial(ffn_bwd_kernel, steps, first),
        grid=(steps + 4,),
        in_specs=[
            rows_of(width),
            slab(2 * units),
            slab(units),
            pl.BlockSpec((quarter, tok), feature),
            pl.BlockSpec((quarter, tok), feature),
        ]
        + [ANY] * 6
        + ([] if first else [rows_of(width)]),
        out_specs=[
            rows_of(width),
            pl.BlockSpec((quarter, 3 * units), lambda i: (jnp.maximum(i - steps - 2, 0), 0)),
            pl.BlockSpec((quarter, 3 * units), lambda i: (jnp.clip(i - steps, 0, 1), 0)),
        ],
        out_shape=[
            shape_of((tok, width), F32),
            shape_of((width // 2, 3 * units), BF16),
            shape_of((width // 2, 3 * units), BF16),
        ],
        scratch_shapes=[
            pltpu.VMEM((width, 2 * units), BF16),
            pltpu.VMEM((width, units), BF16),
            pltpu.VMEM((tok, 2 * units), BF16),
            pltpu.VMEM((tok, units), BF16),
            pltpu.SemaphoreType.DMA((2,)),
        ],
        input_output_aliases={} if first else {11: 0},
        compiler_params=settings(1, 56),
        cost_estimate=cost(2 * tok * width * units * 6, 32 << 20),
        name="ffn_bwd",
    )(low, acts, hiddens, xt, lowt, *pieces, *([] if first else [total]))


def after(value, *others):
    return lax.optimization_barrier((value,) + others)[0]


def z_gather(block):
    one = lax.ppermute(block, "tp", Z_UP)
    three = lax.ppermute(block, "tp", Z_DOWN)
    two = lax.ppermute(one, "tp", Z_UP)
    return [block, one, two, three]


def add(left, right):
    return left.astype(F32) + right.astype(F32)


def add_low(left, right):
    return add(left, right).astype(BF16)


def turn_chunks(block):
    wide = block.shape[1] * 2 // 9
    thin = wide // 2
    starts = [(2 * wide, wide), (wide, wide), (0, wide)]
    starts += [(3 * wide + 2 * thin, thin), (3 * wide + thin, thin), (3 * wide, thin)]
    return jnp.concatenate([block[:, a : a + n] for a, n in starts], axis=1)


def z_reduce(parts):
    two = add_low(parts[1], lax.ppermute(parts[2], "tp", Z_DOWN))
    total = add(parts[0], lax.ppermute(two, "tp", Z_DOWN))
    return total + lax.ppermute(parts[3], "tp", Z_UP).astype(F32)


def per_device_rows(
    tokens,
    teacher,
    lengths,
    attn_gain,
    q_weight,
    k_weight,
    v_weight,
    q_gain,
    k_gain,
    o_weight,
    ffn_gain,
    gate_weight,
    up_weight,
    down_weight,
):
    z = lax.axis_index("tp")
    ctx = lax.axis_index("ctx")
    fsdp = lax.axis_index("fsdp")
    rows_dev, tok, width = tokens.shape
    quarter = width // 4
    hd = q_gain.shape[0] * 4
    q_cols, k_cols = q_weight.shape[1], k_weight.shape[1]
    proj = q_cols + 2 * k_cols
    heads = (q_cols // hd, k_cols // hd)
    units = gate_weight.shape[1]
    slots = rows_dev * 4 * tok * 2

    def x_swap(v):
        return lax.ppermute(v, "fsdp", X_SWAP)

    def core_swap(v):
        return lax.ppermute(v, "fsdp", CORE_SWAP)

    def y_swap(v):
        return lax.ppermute(v, "ctx", Y_SWAP)

    length = lax.dynamic_slice_in_dim(lengths, z, 1, 0)
    info = jnp.concatenate([jnp.stack([z, fsdp, ctx]).astype(jnp.int32), length])

    w_attn, w_ffn = pack(
        info, q_weight, k_weight, v_weight, o_weight, gate_weight, up_weight, down_weight
    )
    count_here = jnp.sum(lengths).astype(F32)[None]
    vector = jnp.concatenate([attn_gain, ffn_gain, q_gain, k_gain]).astype(F32)
    vector = jnp.concatenate([vector, count_here, jnp.zeros((640 - 545,), F32)])[None]
    vector = jnp.concatenate([vector, x_swap(vector)], axis=0)
    vector = jnp.concatenate([vector, core_swap(vector)], axis=0)
    gain_one = vector[:, :quarter].reshape(1, width)
    gain_two = vector[:, quarter : 2 * quarter].reshape(1, width)
    total_count = jnp.sum(vector[:, 544])
    head_gains = vector[:, 2 * quarter : 544]
    head_gains = jnp.where(fsdp // 2 == 0, head_gains, head_gains[jnp.array([1, 0, 3, 2])])
    head_gains = jnp.where(fsdp % 2 == 0, head_gains, head_gains[jnp.array([2, 3, 0, 1])])
    head_gains = head_gains[jnp.array([0, 2, 1, 3])]
    gain_q = head_gains[:, : hd // 4].reshape(hd, 1)
    gain_k = head_gains[:, hd // 4 :].reshape(hd, 1)

    attn_blocks = z_gather(w_attn)
    attn_pieces = []
    for block in attn_blocks:
        far = x_swap(block)
        attn_pieces.append([block, far, core_swap(block), core_swap(far)])
    w_proj = jnp.concatenate([p[:, :proj] for b in attn_pieces for p in b], axis=0)
    w_proj = w_proj.reshape(4, width, proj)
    w_out = jnp.concatenate([p[:, proj:] for b in attn_pieces for p in b], axis=0)
    w_out = w_out.reshape(4, width, q_cols)

    chunk = units
    ffn_blocks = z_gather(after(w_ffn, attn_blocks[2]))
    ffn_pieces = []
    for block in ffn_blocks:
        block = after(block, attn_pieces[2][1]) if block is ffn_blocks[0] else block
        far = x_swap(block[:, : 2 * chunk])
        last = y_swap(far[:, :chunk])
        ffn_pieces.append(
            [block, far, last, core_swap(block), core_swap(far), core_swap(last)]
        )

    x_in, normed_one_t = norm_one(info, tokens, gain_one, 256)
    pos = (ctx * tok + jnp.arange(tok, dtype=jnp.int32)).astype(F32)
    frequency = THETA ** (-(2.0 * jnp.arange(hd // 2, dtype=F32)) / hd)
    angles = frequency[:, None] * pos[None, :]
    tables = (jnp.cos(angles), jnp.sin(angles), gain_q, gain_k)

    def make(block):
        return project(info, w_proj, normed_one_t, *tables, heads, block)

    theirs = [make(lambda s: 2 * (1 - s[2])), make(lambda s: 2 * (1 - s[2]) + 1)]
    got = [y_swap(theirs[0][0]), y_swap(theirs[1][0])]
    mine = [make(lambda s: 2 * s[2]), make(lambda s: 2 * s[2] + 1)]

    outs = [attn_fwd(info, mine[j][0], got[j], hd) for j in range(2)]
    arrived = [y_swap(outs[j][1]) for j in range(2)]
    resid, normed_two, normed_two_t, attended = out_proj(
        info, x_in, [outs[0][0], outs[1][0]], arrived, w_out, gain_two, 256
    )

    order = (0, 1, 3, 2)
    scale = (slots / total_count)[None]
    acts, hiddens, result_low, grad_result, grad_low, grad_low_t, square = ffn_fwd(
        info, scale, normed_two, resid, teacher, [ffn_pieces[k] for k in order], 256
    )

    def spread(block, dtype):
        out = jnp.zeros((rows_dev, tok, width), dtype)
        parts = z_gather(block)
        for k in (0, 1, 3, 2):
            part = parts[k].astype(dtype)[None]
            out = lax.dynamic_update_slice(out, part, (lax.rem(z - k + 4, 4), 0, 0))
        return out

    output = spread(result_low, BF16)

    grad_two = None
    keeps, sends = [None] * 4, [None] * 4
    for k in (2, 1, 3, 0):
        grad_two, keeps[k], sends[k] = ffn_bwd(
            order.index(k),
            grad_low,
            acts,
            hiddens,
            ffn_pieces[k],
            grad_two,
            normed_two_t,
            grad_low_t,
            256,
        )

    def halves(v):
        half = v.shape[0] // 2
        return (
            lax.dynamic_slice_in_dim(v, ctx * half, half, 0),
            lax.dynamic_slice_in_dim(v, half - ctx * half, half, 0),
        )

    def core_sum(keep, send):
        came = core_swap(send)
        return add_low(keep[:quarter], came[:quarter]), add_low(keep[quarter:], came[quarter:])

    def plane_sum(own, far, x_first, turn):
        if x_first:
            own = add_low(own, x_swap(far))
            here, there = halves(own)
            return add_low(here, turn(y_swap(there)))
        here, there = halves(own)
        far_here, far_there = halves(far)
        came = turn(y_swap(jnp.concatenate([there, far_there], axis=0)))
        half = quarter // 2
        return add_low(
            add_low(here, came[:half]), x_swap(add_low(far_here, came[half:]))
        )

    def finish(parts, turn):
        own = z_reduce(parts)
        other = turn(y_swap(own))
        return jnp.concatenate(
            [jnp.where(ctx == 0, own, other), jnp.where(ctx == 0, other, own)], axis=0
        )

    ffn_parts = [
        plane_sum(*core_sum(keeps[k], sends[k]), k in (1, 2), turn_chunks) for k in range(4)
    ]

    grad_resid, grad_attn_t, a0, a1, b0, b1, gain_two_sum = norm_two_back(
        info, grad_two, resid, grad_result, gain_two, w_out, 256
    )

    grad_got = [y_swap(b0), y_swap(b1)]
    grads = [
        attn_bwd(
            info,
            mine[j][0],
            got[j],
            outs[j][0],
            outs[j][1],
            (a0, a1)[j],
            grad_got[j],
            outs[j][2],
            hd,
        )
        for j in range(2)
    ]
    back = [
        head_back(
            info, grads[j][0], y_swap(grads[j][1]), mine[j][1], theirs[j][1], *tables, heads
        )
        for j in range(2)
    ]
    tokens_low, gain_one_sum = norm_one_back(
        info, [back[0][0], back[1][0]], w_proj, x_in, grad_resid, gain_one, 256
    )
    tokens_grad = spread(tokens_low, F32)

    attn_parts = []
    for k in range(4):
        part = jnp.concatenate(
            [
                dot(normed_one_t, back[k % 2][0][k // 2], 1, 0).astype(BF16),
                dot(grad_attn_t, attended[k], 1, 0).astype(BF16),
            ],
            axis=1,
        )
        own, far = core_sum(part[: width // 2], part[width // 2 :])
        attn_parts.append(plane_sum(own, far, k in (1, 2), lambda v: v))

    ffn_grad = finish(ffn_parts, turn_chunks)
    attn_grad = finish(attn_parts, lambda v: v)

    def total(v):
        for axis, pairs in (("fsdp", CORE_SWAP), ("fsdp", X_SWAP), ("ctx", Y_SWAP)):
            v = v + lax.ppermute(v, axis, pairs)
        for pairs in (Z_NEAR, Z_FAR):
            v = v + lax.ppermute(v, "tp", pairs)
        return v

    def natural(v):
        v = v.reshape(4, quarter)[jnp.array([0, 2, 1, 3])]
        v = jnp.where(fsdp % 2 == 0, v, v[jnp.array([1, 0, 3, 2])])
        return jnp.where(fsdp // 2 == 0, v, v[jnp.array([2, 3, 0, 1])]).reshape(1, width)

    gain_heads = back[0][1] + back[1][1]
    sums = total(
        jnp.concatenate(
            [
                natural(gain_one_sum),
                natural(gain_two_sum),
                gain_heads[:, 0].reshape(1, hd),
                gain_heads[:, 1].reshape(1, hd),
                jnp.sum(square).reshape(1, 1),
                jnp.zeros((1, 127), F32),
            ],
            axis=1,
        )
    )[0]
    teacher_loss = sums[2 * width + 2 * hd] / (total_count * width)

    def own_part(at, size):
        return lax.dynamic_slice_in_dim(sums, at + fsdp * (size // 4), size // 4, 0)

    third = units // 3

    def columns(first):
        starts = [first(j) for j in range(3)]
        parts = [ffn_grad[:, s : s + third] for s in starts]
        return jnp.concatenate(
            [jnp.where(ctx == 0, parts[0], parts[2]), parts[1], jnp.where(ctx == 0, parts[2], parts[0])],
            axis=1,
        )

    return (
        output,
        teacher_loss,
        tokens_grad,
        own_part(0, width),
        attn_grad[:, :q_cols],
        attn_grad[:, q_cols : q_cols + k_cols],
        attn_grad[:, q_cols + k_cols : proj],
        own_part(2 * width, hd),
        own_part(2 * width + hd, hd),
        attn_grad[:, proj:].T,
        own_part(width, width),
        columns(lambda j: 2 * j * third),
        columns(lambda j: (2 * j + 1) * third),
        columns(lambda j: 2 * units + j * third).T,
    )


def solution(mesh):
    return jax.shard_map(
        per_device_rows if fits(mesh) else per_device_any,
        mesh=mesh,
        in_specs=(
            P("fsdp", "ctx", None),
            P("fsdp", "ctx", None),
            P("fsdp"),
            P("fsdp"),
            P("fsdp", "tp"),
            P("fsdp", "tp"),
            P("fsdp", "tp"),
            P("fsdp"),
            P("fsdp"),
            P("tp", "fsdp"),
            P("fsdp"),
            P("fsdp", "tp"),
            P("fsdp", "tp"),
            P("tp", "fsdp"),
        ),
        out_specs=(
            P("fsdp", "ctx", None),
            P(),
            P("fsdp", "ctx", None),
            P("fsdp"),
            P("fsdp", "tp"),
            P("fsdp", "tp"),
            P("fsdp", "tp"),
            P("fsdp"),
            P("fsdp"),
            P("tp", "fsdp"),
            P("fsdp"),
            P("fsdp", "tp"),
            P("fsdp", "tp"),
            P("tp", "fsdp"),
        ),
        check_vma=False,
    )
```

```python
import functools
import math

import jax
import jax.numpy as jnp
from jax import lax
from jax.experimental import pallas as pl
from jax.experimental.pallas import tpu as pltpu
from jax.sharding import PartitionSpec as P

EPS = 1e-05
THETA = 1000000.0
NEGATIVE = -1e30


def rms_scale(field_in, gain_vec):
    return (
        field_in * lax.rsqrt(jnp.mean(field_in * field_in, axis=-1, keepdims=True) + EPS) * gain_vec
    )


def rotate(field_in, positions):
    half_dim = field_in.shape[-1] // 2
    frequency = THETA ** (-(2.0 * jnp.arange(half_dim, dtype=jnp.float32)) / field_in.shape[-1])
    angles = positions[:, None] * frequency[None, :]
    cos_part = jnp.cos(angles)[:, None, :]
    sin_part = jnp.sin(angles)[:, None, :]
    lower_half = field_in[..., :half_dim]
    upper_half = field_in[..., half_dim:]
    return jnp.concatenate(
        [
            lower_half * cos_part - upper_half * sin_part,
            upper_half * cos_part + lower_half * sin_part,
        ],
        axis=-1,
    )


def linear(left_mat, right_mat):
    return jnp.dot(left_mat, right_mat, preferred_element_type=jnp.float32)


def linear_left(left_mat, right_mat):
    return lax.dot_general(
        left_mat, right_mat, (((0,), (0,)), ((), ())), preferred_element_type=jnp.float32
    )


def linear_right(left_mat, right_mat):
    return lax.dot_general(
        left_mat, right_mat, (((1,), (1,)), ((), ())), preferred_element_type=jnp.float32
    )


def swiglu(gate_act, up_act):
    return jax.nn.silu(gate_act) * up_act


def per_device_any(
    tokens,
    teacher,
    lengths,
    attn_gain,
    q_weight,
    k_weight,
    v_weight,
    q_gain,
    k_gain,
    o_weight,
    ffn_gain,
    gate_weight,
    up_weight,
    down_weight,
):
    (
        gain_one,
        w_query,
        w_key,
        w_value,
        gain_query,
        gain_key,
        w_output,
        gain_two,
        w_gate,
        w_upper,
        w_down,
    ) = (
        lax.all_gather(attn_gain, "fsdp", axis=0, tiled=True),
        lax.all_gather(q_weight, "fsdp", axis=0, tiled=True),
        lax.all_gather(k_weight, "fsdp", axis=0, tiled=True),
        lax.all_gather(v_weight, "fsdp", axis=0, tiled=True),
        lax.all_gather(q_gain, "fsdp", axis=0, tiled=True),
        lax.all_gather(k_gain, "fsdp", axis=0, tiled=True),
        lax.all_gather(o_weight, "fsdp", axis=1, tiled=True),
        lax.all_gather(ffn_gain, "fsdp", axis=0, tiled=True),
        lax.all_gather(gate_weight, "fsdp", axis=0, tiled=True),
        lax.all_gather(up_weight, "fsdp", axis=0, tiled=True),
        lax.all_gather(down_weight, "fsdp", axis=1, tiled=True),
    )
    rows_dev, block_len, model_width = tokens.shape
    count_tok = rows_dev * block_len
    head_dim = gain_query.shape[0]
    q_heads = w_query.shape[1] // head_dim
    kv_heads = w_key.shape[1] // head_dim
    group_size = q_heads // kv_heads
    score_scale = head_dim ** (-0.5)
    row_len = block_len * lax.axis_size("ctx")
    key_block = math.gcd(row_len, 512)
    block_start = lax.axis_index("ctx") * block_len
    tiles_used = (block_start + block_len + key_block - 1) // key_block
    slot_pos = block_start + jnp.arange(block_len, dtype=jnp.int32)
    positions = slot_pos.astype(jnp.float32)
    valid = (slot_pos[None, :] < lengths[:, None]).astype(jnp.float32)
    slots = count_tok * lax.axis_size("fsdp") * lax.axis_size("ctx")
    gain_two_f = gain_two.astype(jnp.float32)
    gain_one_f = gain_one.astype(jnp.float32)
    inputs = tokens.astype(jnp.float32)
    normed_one, back_one = jax.vjp(rms_scale, inputs, gain_one_f)
    normed_low = normed_one.astype(jnp.bfloat16).reshape(count_tok, model_width)
    query_raw = linear(normed_low, w_query)
    key_raw = linear(normed_low, w_key)
    value_raw = linear(normed_low, w_value)

    def heads_post(raw_heads, gain_vec):
        shaped = raw_heads.reshape(rows_dev, block_len, -1, head_dim)
        return rotate(rms_scale(shaped, gain_vec), positions)

    query_rot, query_back = jax.vjp(heads_post, query_raw, gain_query.astype(jnp.float32))
    key_rot, key_back = jax.vjp(heads_post, key_raw, gain_key.astype(jnp.float32))
    queries = query_rot.astype(jnp.bfloat16).reshape(
        rows_dev, block_len, kv_heads, group_size, head_dim
    )
    key_rows = key_rot.astype(jnp.bfloat16).reshape(rows_dev, block_len, kv_heads * head_dim)
    values = value_raw.astype(jnp.bfloat16).reshape(rows_dev, block_len, kv_heads * head_dim)
    keys_all, values_all = (
        lax.all_gather(key_rows, "ctx", axis=1, tiled=True),
        lax.all_gather(values, "ctx", axis=1, tiled=True),
    )

    def key_tile(tile_index):
        tile_start = tile_index * key_block
        key_pos = tile_start + jnp.arange(key_block, dtype=jnp.int32)
        key_part = lax.dynamic_slice_in_dim(keys_all, tile_start, key_block, 1).reshape(
            rows_dev, key_block, kv_heads, head_dim
        )
        value_part = lax.dynamic_slice_in_dim(values_all, tile_start, key_block, 1).reshape(
            rows_dev, key_block, kv_heads, head_dim
        )
        scores = (
            jnp.einsum("rqhgd,rkhd->rhgqk", queries, key_part, preferred_element_type=jnp.float32)
            * score_scale
        )
        allowed = (key_pos[None, None, :] <= slot_pos[None, :, None]) & (
            key_pos[None, None, :] < lengths[:, None, None]
        )
        return (tile_start, scores, allowed[:, None, None], key_part, value_part)

    stat_shape = (rows_dev, kv_heads, group_size, block_len)

    def stats_step(tile_index, carried):
        running_max, running_sum = carried
        tile_start, scores, allowed, key_part, value_part = key_tile(tile_index)
        masked = jnp.where(allowed, scores, NEGATIVE)
        new_max = jnp.maximum(running_max, jnp.max(masked, axis=-1))
        terms = jnp.where(allowed, jnp.exp(masked - new_max[..., None]), 0.0)
        return (new_max, running_sum * jnp.exp(running_max - new_max) + jnp.sum(terms, axis=-1))

    running_max, running_sum = lax.fori_loop(
        0,
        tiles_used,
        stats_step,
        (jnp.full(stat_shape, NEGATIVE, jnp.float32), jnp.zeros(stat_shape, jnp.float32)),
    )
    log_total = running_max + jnp.log(running_sum)
    out_shape = (rows_dev, block_len, kv_heads, group_size, head_dim)

    def value_step(tile_index, carried):
        rounded_out, exact_out = carried
        tile_start, scores, allowed, key_part, value_part = key_tile(tile_index)
        tile_probs = jnp.where(allowed, jnp.exp(scores - log_total[..., None]), 0.0)
        rounded_out = rounded_out + jnp.einsum(
            "rhgqk,rkhd->rqhgd",
            tile_probs.astype(jnp.bfloat16),
            value_part,
            preferred_element_type=jnp.float32,
        )
        exact_out = exact_out + jnp.einsum(
            "rhgqk,rkhd->rqhgd", tile_probs, value_part.astype(jnp.float32)
        )
        return (rounded_out, exact_out)

    rounded_out, exact_out = lax.fori_loop(
        0,
        tiles_used,
        value_step,
        (jnp.zeros(out_shape, jnp.float32), jnp.zeros(out_shape, jnp.float32)),
    )
    attended = rounded_out.astype(jnp.bfloat16).reshape(count_tok, q_heads * head_dim)
    attn_total = lax.psum(linear(attended, w_output), "tp")
    resid = inputs + attn_total.reshape(rows_dev, block_len, model_width)
    normed_two, back_two = jax.vjp(rms_scale, resid, gain_two_f)
    normed_second = normed_two.astype(jnp.bfloat16).reshape(count_tok, model_width)
    gate_act = linear(normed_second, w_gate)
    up_act = linear(normed_second, w_upper)
    hidden_full, back_glu = jax.vjp(swiglu, gate_act, up_act)
    hidden = hidden_full.astype(jnp.bfloat16)
    ffn_total = lax.psum(linear(hidden, w_down), "tp")
    result = resid + ffn_total.reshape(rows_dev, block_len, model_width)
    error_value = result - teacher.astype(jnp.float32)
    valid_col = valid[..., None]
    total_square, total_count = lax.psum(
        (jnp.sum(valid_col * error_value * error_value), jnp.sum(valid)), ("fsdp", "ctx")
    )
    teacher_loss = total_square / (total_count * model_width)
    grad_result = valid_col * error_value * (slots / total_count)
    grad_low = grad_result.astype(jnp.bfloat16).reshape(count_tok, model_width)
    grad_down = linear_left(hidden, grad_low)
    grad_hidden = linear_right(grad_low, w_down)
    grad_gate_full, grad_up_full = back_glu(grad_hidden)
    grad_gate = grad_gate_full.astype(jnp.bfloat16)
    grad_up = grad_up_full.astype(jnp.bfloat16)
    grad_wgate = linear_left(normed_second, grad_gate)
    grad_wup = linear_left(normed_second, grad_up)
    normed_two_part = linear_right(grad_gate, w_gate) + linear_right(grad_up, w_upper)
    grad_normed_two = lax.psum(normed_two_part, "tp")
    grad_resid_norm, grad_gain_two = back_two(
        grad_normed_two.reshape(rows_dev, block_len, model_width)
    )
    grad_resid = grad_result + grad_resid_norm
    grad_attn_low = grad_resid.astype(jnp.bfloat16).reshape(count_tok, model_width)
    grad_woutput = linear_left(attended, grad_attn_low)
    grad_attended = linear_right(grad_attn_low, w_output).astype(jnp.bfloat16).reshape(out_shape)
    delta = jnp.einsum("rqhgd,rqhgd->rhgq", grad_attended.astype(jnp.float32), exact_out)
    full_shape = (rows_dev, row_len, kv_heads * head_dim)

    def grad_step(tile_index, carried):
        grad_queries, grad_keys, grad_values = carried
        tile_start, scores, allowed, key_part, value_part = key_tile(tile_index)
        tile_probs = jnp.where(allowed, jnp.exp(scores - log_total[..., None]), 0.0)
        grad_probs = jnp.einsum(
            "rqhgd,rkhd->rhgqk", grad_attended, value_part, preferred_element_type=jnp.float32
        )
        grad_scores = (tile_probs * (grad_probs - delta[..., None])).astype(jnp.bfloat16)
        grad_queries = (
            grad_queries
            + jnp.einsum(
                "rhgqk,rkhd->rqhgd", grad_scores, key_part, preferred_element_type=jnp.float32
            )
            * score_scale
        )
        key_term = (
            jnp.einsum(
                "rhgqk,rqhgd->rkhd", grad_scores, queries, preferred_element_type=jnp.float32
            )
            * score_scale
        )
        value_term = jnp.einsum(
            "rhgqk,rqhgd->rkhd",
            tile_probs.astype(jnp.bfloat16),
            grad_attended,
            preferred_element_type=jnp.float32,
        )
        grad_keys = lax.dynamic_update_slice_in_dim(
            grad_keys, key_term.reshape(rows_dev, key_block, kv_heads * head_dim), tile_start, 1
        )
        grad_values = lax.dynamic_update_slice_in_dim(
            grad_values, value_term.reshape(rows_dev, key_block, kv_heads * head_dim), tile_start, 1
        )
        return (grad_queries, grad_keys, grad_values)

    grad_queries, grad_keys, grad_values = lax.fori_loop(
        0,
        tiles_used,
        grad_step,
        (
            jnp.zeros(out_shape, jnp.float32),
            jnp.zeros(full_shape, jnp.float32),
            jnp.zeros(full_shape, jnp.float32),
        ),
    )
    key_grad, value_grad = (
        lax.psum_scatter(grad_keys, "ctx", scatter_dimension=1, tiled=True),
        lax.psum_scatter(grad_values, "ctx", scatter_dimension=1, tiled=True),
    )
    grad_query_raw, grad_gain_query = query_back(
        grad_queries.reshape(rows_dev, block_len, q_heads, head_dim)
    )
    grad_key_raw, grad_gain_key = key_back(
        key_grad.reshape(rows_dev, block_len, kv_heads, head_dim)
    )
    query_low = grad_query_raw.astype(jnp.bfloat16)
    key_low = grad_key_raw.astype(jnp.bfloat16)
    value_low = value_grad.reshape(count_tok, kv_heads * head_dim).astype(jnp.bfloat16)
    grad_wquery = linear_left(normed_low, query_low)
    grad_wkey = linear_left(normed_low, key_low)
    grad_wvalue = linear_left(normed_low, value_low)
    normed_part = (
        linear_right(query_low, w_query)
        + linear_right(key_low, w_key)
        + linear_right(value_low, w_value)
    )
    grad_normed_one, grad_gain_query, grad_gain_key = lax.psum(
        (normed_part, grad_gain_query, grad_gain_key), "tp"
    )
    grad_input_norm, grad_gain_one = back_one(
        grad_normed_one.reshape(rows_dev, block_len, model_width)
    )
    tokens_grad = grad_resid + grad_input_norm
    partials = (
        grad_gain_one,
        grad_wquery,
        grad_wkey,
        grad_wvalue,
        grad_gain_query,
        grad_gain_key,
        grad_woutput,
        grad_gain_two,
        grad_wgate,
        grad_wup,
        grad_down,
    )
    pieces = (
        lax.psum_scatter(partials[0], ("fsdp", "ctx"), scatter_dimension=0, tiled=True),
        lax.psum_scatter(partials[1], ("fsdp", "ctx"), scatter_dimension=0, tiled=True),
        lax.psum_scatter(partials[2], ("fsdp", "ctx"), scatter_dimension=0, tiled=True),
        lax.psum_scatter(partials[3], ("fsdp", "ctx"), scatter_dimension=0, tiled=True),
        lax.psum_scatter(partials[4], ("fsdp", "ctx"), scatter_dimension=0, tiled=True),
        lax.psum_scatter(partials[5], ("fsdp", "ctx"), scatter_dimension=0, tiled=True),
        lax.psum_scatter(partials[6], ("fsdp", "ctx"), scatter_dimension=1, tiled=True),
        lax.psum_scatter(partials[7], ("fsdp", "ctx"), scatter_dimension=0, tiled=True),
        lax.psum_scatter(partials[8], ("fsdp", "ctx"), scatter_dimension=0, tiled=True),
        lax.psum_scatter(partials[9], ("fsdp", "ctx"), scatter_dimension=0, tiled=True),
        lax.psum_scatter(partials[10], ("fsdp", "ctx"), scatter_dimension=1, tiled=True),
    )
    summed = (
        lax.all_gather(pieces[0], "ctx", axis=0, tiled=True),
        lax.all_gather(pieces[1], "ctx", axis=0, tiled=True),
        lax.all_gather(pieces[2], "ctx", axis=0, tiled=True),
        lax.all_gather(pieces[3], "ctx", axis=0, tiled=True),
        lax.all_gather(pieces[4], "ctx", axis=0, tiled=True),
        lax.all_gather(pieces[5], "ctx", axis=0, tiled=True),
        lax.all_gather(pieces[6], "ctx", axis=1, tiled=True),
        lax.all_gather(pieces[7], "ctx", axis=0, tiled=True),
        lax.all_gather(pieces[8], "ctx", axis=0, tiled=True),
        lax.all_gather(pieces[9], "ctx", axis=0, tiled=True),
        lax.all_gather(pieces[10], "ctx", axis=1, tiled=True),
    )
    return (
        result.astype(jnp.bfloat16),
        teacher_loss,
        tokens_grad,
        summed[0],
        summed[1],
        summed[2],
        summed[3],
        summed[4],
        summed[5],
        summed[6],
        summed[7],
        summed[8],
        summed[9],
        summed[10],
    )


BF16 = jnp.bfloat16
F32 = jnp.float32
LOG2E = math.log2(math.e)
X_SWAP = [(0, 2), (2, 0), (1, 3), (3, 1)]
CORE_SWAP = [(0, 1), (1, 0), (2, 3), (3, 2)]
Y_SWAP = [(0, 1), (1, 0)]
Z_UP = [(0, 1), (1, 2), (2, 3), (3, 0)]
Z_DOWN = [(0, 3), (1, 0), (2, 1), (3, 2)]
Z_NEAR = [(0, 1), (1, 0), (2, 3), (3, 2)]
Z_FAR = [(0, 2), (2, 0), (1, 3), (3, 1)]
MASKS = (0, 2, 1, 3)
ANY = pl.BlockSpec(memory_space=pl.ANY)
SMEM = pl.BlockSpec(memory_space=pltpu.SMEM)


def fits(mesh):
    return dict(mesh.shape) == {"fsdp": 4, "ctx": 2, "tp": 4}


def dot(left, right, left_dim, right_dim):
    return lax.dot_general(
        left, right, (((left_dim,), (right_dim,)), ((), ())), preferred_element_type=F32
    )


def sigmoid(v):
    return 0.5 * jnp.tanh(0.5 * v) + 0.5


def whole(shape):
    zeros = (0,) * len(shape)
    return pl.BlockSpec(shape, lambda *_: zeros, pipeline_mode=pl.Buffered(1))


def settings(dims, mib):
    return pltpu.CompilerParams(
        dimension_semantics=("arbitrary",) * dims, vmem_limit_bytes=mib << 20
    )


def shape_of(shape, dtype):
    return jax.ShapeDtypeStruct(shape, dtype)


def cost(flops, bytes_accessed):
    return pl.CostEstimate(flops=flops >> 8, bytes_accessed=bytes_accessed >> 8, transcendentals=0)


def pack_kernel(info, q_ref, k_ref, v_ref, o_ref, g_ref, u_ref, d_ref, attn_ref, ffn_ref):
    ctx = info[2]
    q_cols, k_cols = q_ref.shape[1], k_ref.shape[1]
    attn_ref[:, :q_cols] = q_ref[...]
    attn_ref[:, q_cols : q_cols + k_cols] = k_ref[...]
    attn_ref[:, q_cols + k_cols : q_cols + 2 * k_cols] = v_ref[...]
    attn_ref[:, q_cols + 2 * k_cols :] = o_ref[...].astype(F32).T.astype(BF16)
    third = g_ref.shape[1] // 3
    for j in range(3):
        at = pl.multiple_of(jnp.where(ctx == 0, j, 2 - j) * third, third)
        base = 3 * third * j
        ffn_ref[:, base : base + third] = g_ref[:, pl.ds(at, third)]
        ffn_ref[:, base + third : base + 2 * third] = u_ref[:, pl.ds(at, third)]
        down = d_ref[pl.ds(at, third), :].astype(F32).T.astype(BF16)
        ffn_ref[:, base + 2 * third : base + 3 * third] = down


def pack(info, q, k, v, o, g, u, d):
    rows = q.shape[0]
    attn_cols = q.shape[1] + 2 * k.shape[1] + o.shape[0]
    return pl.pallas_call(
        pack_kernel,
        in_specs=[SMEM] + [pl.BlockSpec(memory_space=pltpu.VMEM)] * 7,
        out_specs=[pl.BlockSpec(memory_space=pltpu.VMEM)] * 2,
        out_shape=[shape_of((rows, attn_cols), BF16), shape_of((rows, 3 * g.shape[1]), BF16)],
        compiler_params=pltpu.CompilerParams(vmem_limit_bytes=24 << 20),
        cost_estimate=cost(0, 6 << 20),
        name="pack",
    )(info, q, k, v, o, g, u, d)


def norm_one_kernel(info, tok_ref, gain_ref, x_ref, nt_ref, x32):
    quarter = x_ref.shape[1] // 4
    for p, mask in enumerate(MASKS):
        at = pl.multiple_of(jnp.bitwise_xor(info[1], mask) * quarter, quarter)
        part = tok_ref[0, :, pl.ds(at, quarter)]
        x_ref[:, p * quarter : (p + 1) * quarter] = part
        x32[:, p * quarter : (p + 1) * quarter] = part.astype(F32)
    x = x32[...]
    rho = lax.rsqrt(jnp.mean(x * x, axis=-1, keepdims=True) + EPS)
    nt_ref[...] = (x * rho * gain_ref[...]).T.astype(BF16)


def norm_one(info, tokens, gain, tile):
    _, tok, width = tokens.shape
    return pl.pallas_call(
        norm_one_kernel,
        grid_spec=pltpu.PrefetchScalarGridSpec(
            num_scalar_prefetch=1,
            grid=(tok // tile,),
            in_specs=[
                pl.BlockSpec((1, tile, width), lambda i, info: (info[0], i, 0)),
                pl.BlockSpec((1, width), lambda i, info: (0, 0)),
            ],
            out_specs=[
                pl.BlockSpec((tile, width), lambda i, info: (i, 0)),
                pl.BlockSpec((width, tile), lambda i, info: (0, i)),
            ],
            scratch_shapes=[pltpu.VMEM((tile, width), F32)],
        ),
        out_shape=[shape_of((tok, width), BF16), shape_of((width, tok), BF16)],
        compiler_params=settings(1, 24),
        cost_estimate=cost(0, 6 << 20),
        name="norm_one",
    )(info, tokens, gain)


def proj_kernel(heads, info, w_ref, nt_ref, cos_ref, sin_ref, qg_ref, kg_ref, rot_ref, raw_ref):
    hd = qg_ref.shape[0]
    tok = nt_ref.shape[1]
    half = hd // 2
    raw = dot(w_ref[0], nt_ref[...], 0, 0)
    cos_part, sin_part = cos_ref[...], sin_ref[...]
    heads_q, heads_k = heads
    raw_ref[...] = raw.astype(BF16)
    for h in range(heads_q + heads_k):
        v = raw[h * hd : (h + 1) * hd]
        rho = lax.rsqrt(jnp.mean(v * v, axis=0, keepdims=True) + EPS)
        v = v * rho * (qg_ref[...] if h < heads_q else kg_ref[...])
        a, b = v[:half], v[half:]
        rot_ref[h * hd : h * hd + half, :] = (a * cos_part - b * sin_part).astype(BF16)
        rot_ref[h * hd + half : (h + 1) * hd, :] = (b * cos_part + a * sin_part).astype(BF16)
    at = (heads_q + heads_k) * hd
    rot_ref[at:, :] = raw[at:].astype(BF16)


def project(info, w_proj, normed_t, cos_part, sin_part, gain_q, gain_k, heads, block):
    _, width, cols = w_proj.shape
    tok = normed_t.shape[1]
    tile = min(512, tok)
    const = lambda a: pl.BlockSpec(a.shape, lambda i, info: (0, 0))
    tab = lambda a: pl.BlockSpec((a.shape[0], tile), lambda i, info: (0, i))
    return pl.pallas_call(
        functools.partial(proj_kernel, heads),
        grid_spec=pltpu.PrefetchScalarGridSpec(
            num_scalar_prefetch=1,
            grid=(tok // tile,),
            in_specs=[
                pl.BlockSpec((1, width, cols), lambda i, info: (block(info), 0, 0)),
                tab(normed_t),
                tab(cos_part),
                tab(sin_part),
                const(gain_q),
                const(gain_k),
            ],
            out_specs=[pl.BlockSpec((cols, tile), lambda i, info: (0, i))] * 2,
        ),
        out_shape=[shape_of((cols, tok), BF16), shape_of((cols, tok), BF16)],
        compiler_params=settings(1, 24),
        cost_estimate=cost(2 * width * cols * tok, 6 << 20),
        name="project",
    )(info, w_proj, normed_t, cos_part, sin_part, gain_q, gain_k)


def head_back_kernel(
    heads, info, dm_ref, dt_ref, rm_ref, rt_ref, cos_ref, sin_ref, qg_ref, kg_ref, out_ref, gg_ref
):
    step, part = pl.program_id(0), pl.program_id(1)
    hd = qg_ref.shape[0]
    half = hd // 2
    heads_q, heads_k = heads
    cos_part, sin_part = cos_ref[...], sin_ref[...]
    tile = cos_part.shape[1]

    @pl.when((step == 0) & (part == 0))
    def _():
        gg_ref[...] = jnp.zeros_like(gg_ref)

    def work(d_ref, r_ref):
        gain_q = jnp.zeros((hd, 1), F32)
        gain_k = jnp.zeros((hd, 1), F32)
        done = []
        for h in range(heads_q + heads_k):
            is_q = h < heads_q
            g = d_ref[h * hd : (h + 1) * hd, :].astype(F32)
            raw = r_ref[h * hd : (h + 1) * hd, :].astype(F32)
            a, b = g[:half], g[half:]
            turned = jnp.concatenate(
                [a * cos_part + b * sin_part, b * cos_part - a * sin_part], axis=0
            )
            rho = lax.rsqrt(jnp.mean(raw * raw, axis=0, keepdims=True) + EPS)
            unit = raw * rho
            prod = turned * unit
            scaled = turned * (qg_ref[...] if is_q else kg_ref[...])
            mean = jnp.mean(scaled * unit, axis=0, keepdims=True)
            done.append(rho * (scaled - unit * mean))
            total = jnp.sum(prod, axis=1, keepdims=True)
            if is_q:
                gain_q = gain_q + total
            else:
                gain_k = gain_k + total
        done.append(d_ref[(heads_q + heads_k) * hd :, :].astype(F32))
        out_ref[0] = jnp.concatenate(done, axis=0).T.astype(BF16)
        lane = lax.broadcasted_iota(jnp.int32, gg_ref.shape, 1)
        gg_ref[...] += jnp.where(lane == 0, gain_q, jnp.where(lane == 1, gain_k, 0.0))

    @pl.when(step == 0)
    def _():
        work(dm_ref, rm_ref)

    @pl.when(step == 1)
    def _():
        work(dt_ref, rt_ref)


def head_back(info, grad_mine, grad_theirs, raw_mine, raw_theirs, cos_part, sin_part, gq, gk, heads):
    cols, tok = grad_mine.shape
    tile = min(512, tok)
    mine = pl.BlockSpec((cols, tile), lambda s, i, info: (0, jnp.where(s == 0, i, tok // tile - 1)))
    theirs = pl.BlockSpec((cols, tile), lambda s, i, info: (0, jnp.where(s == 0, 0, i)))
    tab = lambda a: pl.BlockSpec((a.shape[0], tile), lambda s, i, info: (0, i))
    const = lambda a: pl.BlockSpec(a.shape, lambda s, i, info: (0, 0))
    return pl.pallas_call(
        functools.partial(head_back_kernel, heads),
        grid_spec=pltpu.PrefetchScalarGridSpec(
            num_scalar_prefetch=1,
            grid=(2, tok // tile),
            in_specs=[
                mine,
                theirs,
                mine,
                theirs,
                tab(cos_part),
                tab(sin_part),
                const(gq),
                const(gk),
            ],
            out_specs=[
                pl.BlockSpec(
                    (1, tile, cols), lambda s, i, info: (jnp.bitwise_xor(info[2], s), i, 0)
                ),
                pl.BlockSpec((gq.shape[0], 128), lambda s, i, info: (0, 0)),
            ],
        ),
        out_shape=[shape_of((2, tok, cols), BF16), shape_of((gq.shape[0], 128), F32)],
        compiler_params=settings(2, 24),
        cost_estimate=cost(0, 8 << 20),
        name="head_back",
    )(info, grad_mine, grad_theirs, raw_mine, raw_theirs, cos_part, sin_part, gq, gk)


def load_rows(info, mine_ref, got_ref, rows, sems):
    tok = mine_ref.shape[1]
    ctx = info[2]
    here = pl.multiple_of(ctx * tok, tok)
    there = pl.multiple_of((1 - ctx) * tok, tok)
    one = pltpu.make_async_copy(mine_ref, rows.at[:, pl.ds(here, tok)], sems.at[0])
    two = pltpu.make_async_copy(got_ref, rows.at[:, pl.ds(there, tok)], sems.at[1])
    one.start()
    two.start()
    one.wait()
    two.wait()


def keys_with_bias(keys, length):
    hd, slots = keys.shape
    pos = lax.broadcasted_iota(jnp.int32, (hd, slots), 1)
    row = lax.broadcasted_iota(jnp.int32, (hd, slots), 0)
    bias = jnp.where((row == 0) & (pos >= length), NEGATIVE, 0.0)
    return jnp.concatenate([keys.astype(F32), bias], axis=0).T.astype(BF16)


def query_with_one(pair):
    one_row = jnp.where(lax.broadcasted_iota(jnp.int32, pair.shape, 0) == 0, 1.0, 0.0)
    return jnp.concatenate([pair, one_row.astype(BF16)], axis=0)


def causal(scores, width):
    key_pos = lax.broadcasted_iota(jnp.int32, (width, width), 0)
    query_pos = lax.broadcasted_iota(jnp.int32, (width, width), 1)
    allowed = key_pos <= query_pos
    return jnp.where(jnp.concatenate([allowed, allowed], axis=1), scores, NEGATIVE)


def attn_fwd_kernel(
    width, hd, info, mine_ref, got_ref, keep_ref, send_ref, lse_ref, rows, key_rows, sems
):
    head, block = pl.program_id(0), pl.program_id(1)
    heads_k = pl.num_programs(0)
    scale = hd**-0.5 * LOG2E
    length = info[3]
    key_at = pl.multiple_of(heads_k * 2 * hd + head * hd, hd)
    value_at = pl.multiple_of(heads_k * 3 * hd + head * hd, hd)
    query_at = pl.multiple_of(head * 2 * hd, 2 * hd)

    @pl.when((head == 0) & (block == 0))
    def _():
        load_rows(info, mine_ref, got_ref, rows, sems)

    @pl.when(block == 0)
    def _():
        key_rows[...] = keys_with_bias(rows[pl.ds(key_at, hd), :], length)

    start = pl.multiple_of(block * width, width)
    both = rows[pl.ds(query_at, 2 * hd), pl.ds(start, width)]
    query = query_with_one(jnp.concatenate([both[:hd], both[hd:]], axis=1))

    def tile(at, carried, diagonal):
        out, total = carried
        scores = dot(key_rows[pl.ds(at, width), :], query, 1, 0)
        if diagonal:
            scores = causal(scores, width)
        probs = jnp.exp2(scores * scale)
        total = total + jnp.sum(probs, axis=0, keepdims=True)
        out = out + dot(rows[pl.ds(value_at, hd), pl.ds(at, width)], probs.astype(BF16), 1, 0)
        return out, total

    carried = (jnp.zeros((hd, 2 * width), F32), jnp.zeros((1, 2 * width), F32))
    full = jnp.minimum(block, lax.div(length + width - 1, width))
    carried = lax.fori_loop(
        0, full, lambda j, c: tile(pl.multiple_of(j * width, width), c, False), carried
    )
    out, total = tile(start, carried, True)
    out = out * (1.0 / total)
    out = jnp.concatenate([out[:, :width], out[:, width:]], axis=0).T.astype(BF16)
    here = block // 2 == info[2]

    @pl.when(here)
    def _():
        keep_ref[...] = out

    @pl.when(jnp.logical_not(here))
    def _():
        send_ref[...] = out

    log_total = jnp.log2(total)
    lse_ref[0, 0:1, :] = log_total[:, :width]
    lse_ref[0, 1:2, :] = log_total[:, width:]


def keep_block(i, info):
    return jnp.clip(i - 2 * info[2], 0, 1)


def send_block(i, info):
    return jnp.clip(i - 2 * (1 - info[2]), 0, 1)


def attn_fwd(info, mine, got, hd):
    cols, tok = mine.shape
    heads_k = cols // (4 * hd)
    width = tok // 2
    return pl.pallas_call(
        functools.partial(attn_fwd_kernel, width, hd),
        grid_spec=pltpu.PrefetchScalarGridSpec(
            num_scalar_prefetch=1,
            grid=(heads_k, 4),
            in_specs=[ANY, ANY],
            out_specs=[
                pl.BlockSpec((width, 2 * hd), lambda h, i, info: (keep_block(i, info), h)),
                pl.BlockSpec((width, 2 * hd), lambda h, i, info: (send_block(i, info), h)),
                pl.BlockSpec((1, 2, width), lambda h, i, info: (h, 0, i)),
            ],
            scratch_shapes=[
                pltpu.VMEM((cols, 2 * tok), BF16),
                pltpu.VMEM((2 * tok, 2 * hd), BF16),
                pltpu.SemaphoreType.DMA((2,)),
            ],
        ),
        out_shape=[
            shape_of((tok, heads_k * 2 * hd), BF16),
            shape_of((tok, heads_k * 2 * hd), BF16),
            shape_of((heads_k, 2, 2 * tok), F32),
        ],
        compiler_params=settings(2, 32),
        cost_estimate=cost(heads_k * 2 * tok * 2 * tok * 256 * 4, 8 << 20),
        name="attn_fwd",
    )(info, mine, got)


def attn_bwd_kernel(
    width,
    hd,
    info,
    mine_ref,
    got_ref,
    ok_ref,
    os_ref,
    gk_ref,
    gs_ref,
    lse_ref,
    keep_ref,
    send_ref,
    rows,
    key_rows,
    value_rows,
    key_sum,
    value_sum,
    sems,
):
    head, block = pl.program_id(0), pl.program_id(1)
    heads_k = pl.num_programs(0)
    scale = hd**-0.5
    length = info[3]
    ctx = info[2]
    tok = keep_ref.shape[1]
    key_at = pl.multiple_of(heads_k * 2 * hd + head * hd, hd)
    value_at = pl.multiple_of(heads_k * 3 * hd + head * hd, hd)
    query_at = pl.multiple_of(head * 2 * hd, 2 * hd)

    @pl.when((head == 0) & (block == 0))
    def _():
        load_rows(info, mine_ref, got_ref, rows, sems)

    @pl.when(block == 0)
    def _():
        key_rows[...] = keys_with_bias(rows[pl.ds(key_at, hd), :], length)
        value_rows[...] = rows[pl.ds(value_at, hd), :].astype(F32).T.astype(BF16)
        key_sum[...] = jnp.zeros_like(key_sum)
        value_sum[...] = jnp.zeros_like(value_sum)

    start = pl.multiple_of(block * width, width)
    here = block // 2 == ctx

    def store_query(value):
        at = pl.ds(pl.multiple_of((block % 2) * width, width), width)

        @pl.when(here)
        def _():
            keep_ref[pl.ds(query_at, 2 * hd), at] = value

        @pl.when(jnp.logical_not(here))
        def _():
            send_ref[pl.ds(query_at, 2 * hd), at] = value

    @pl.when(block * width < length)
    def _():
        both = rows[pl.ds(query_at, 2 * hd), pl.ds(start, width)]
        pair = jnp.concatenate([both[:hd], both[hd:]], axis=1)
        query = query_with_one(pair)
        query_rows = pair.astype(F32).T.astype(BF16)
        grad_wide = jnp.where(here, gk_ref[...].astype(F32), gs_ref[...].astype(F32))
        out_wide = jnp.where(here, ok_ref[...].astype(F32), os_ref[...].astype(F32))
        grad_rows = jnp.concatenate([grad_wide[:, :hd], grad_wide[:, hd:]], axis=0).astype(BF16)
        grad_t = grad_wide.T
        prod = (grad_wide * out_wide).T
        grad = jnp.concatenate([grad_t[:hd], grad_t[hd:]], axis=1).astype(BF16)
        delta = jnp.concatenate(
            [
                jnp.sum(prod[:hd], axis=0, keepdims=True),
                jnp.sum(prod[hd:], axis=0, keepdims=True),
            ],
            axis=1,
        )
        lse = jnp.concatenate([lse_ref[0, 0:1, :], lse_ref[0, 1:2, :]], axis=1)

        def tile(at, query_sum, diagonal):
            scores = dot(key_rows[pl.ds(at, width), :], query, 1, 0)
            if diagonal:
                scores = causal(scores, width)
            probs = jnp.exp2(scores * (scale * LOG2E) - lse)
            grad_probs = dot(value_rows[pl.ds(at, width), :], grad, 1, 0)
            grad_scores = (probs * (grad_probs - delta)).astype(BF16)
            value_sum[pl.ds(at, width), :] += dot(probs.astype(BF16), grad_rows, 1, 0)
            key_sum[pl.ds(at, width), :] += dot(grad_scores, query_rows, 1, 0)
            return query_sum + dot(rows[pl.ds(key_at, hd), pl.ds(at, width)], grad_scores, 1, 0)

        query_sum = lax.fori_loop(
            0,
            block,
            lambda j, s: tile(pl.multiple_of(j * width, width), s, False),
            jnp.zeros((hd, 2 * width), F32),
        )
        query_sum = tile(start, query_sum, True) * scale
        store_query(
            jnp.concatenate([query_sum[:, :width], query_sum[:, width:]], axis=0).astype(BF16)
        )

    @pl.when(block * width >= length)
    def _():
        store_query(jnp.zeros((2 * hd, width), BF16))

    @pl.when(block == 3)
    def _():
        for at, total in ((key_at, key_sum[...] * scale), (value_at, value_sum[...])):
            total = total.T.astype(BF16)
            left, right = total[:, :tok], total[:, tok:]

            @pl.when(ctx == 0)
            def _():
                keep_ref[pl.ds(at, hd), :] = left
                send_ref[pl.ds(at, hd), :] = right

            @pl.when(ctx == 1)
            def _():
                keep_ref[pl.ds(at, hd), :] = right
                send_ref[pl.ds(at, hd), :] = left


def attn_bwd(info, mine, got, out_keep, out_send, grad_keep, grad_send, lse, hd):
    cols, tok = mine.shape
    heads_k = cols // (4 * hd)
    width = tok // 2
    keep = pl.BlockSpec((width, 2 * hd), lambda h, i, info: (keep_block(i, info), h))
    send = pl.BlockSpec((width, 2 * hd), lambda h, i, info: (send_block(i, info), h))
    full = pl.BlockSpec((cols, tok), lambda h, i, info: (0, 0))
    return pl.pallas_call(
        functools.partial(attn_bwd_kernel, width, hd),
        grid_spec=pltpu.PrefetchScalarGridSpec(
            num_scalar_prefetch=1,
            grid=(heads_k, 4),
            in_specs=[
                ANY,
                ANY,
                keep,
                send,
                keep,
                send,
                pl.BlockSpec((1, 2, width), lambda h, i, info: (h, 0, i)),
            ],
            out_specs=[full, full],
            scratch_shapes=[
                pltpu.VMEM((cols, 2 * tok), BF16),
                pltpu.VMEM((2 * tok, 2 * hd), BF16),
                pltpu.VMEM((2 * tok, hd), BF16),
                pltpu.VMEM((2 * tok, hd), F32),
                pltpu.VMEM((2 * tok, hd), F32),
                pltpu.SemaphoreType.DMA((2,)),
            ],
        ),
        out_shape=[shape_of((cols, tok), BF16), shape_of((cols, tok), BF16)],
        compiler_params=settings(2, 40),
        cost_estimate=cost(heads_k * 5 * tok * 2 * tok * 256 * 4, 12 << 20),
        name="attn_bwd",
    )(info, mine, got, out_keep, out_send, grad_keep, grad_send, lse)


def out_proj_kernel(info, x_ref, a0, a1, b0, b1, w_ref, gain_ref, r_ref, n_ref, nt_ref, att_ref):
    ctx = info[2]
    total = x_ref[...].astype(F32)
    for j, ref, side in ((0, a0, ctx), (1, a1, ctx), (0, b0, 1 - ctx), (1, b1, 1 - ctx)):
        block = 2 * side + j
        part = ref[...]
        att_ref[block] = part
        total = total + dot(part, w_ref[block], 1, 1)
    rho = lax.rsqrt(jnp.mean(total * total, axis=-1, keepdims=True) + EPS)
    normed = total * rho * gain_ref[...]
    r_ref[...] = total
    n_ref[...] = normed.astype(BF16)
    nt_ref[...] = normed.T.astype(BF16)


def out_proj(info, x, mine, theirs, w_out, gain, tile):
    tok, width = x.shape
    feats = w_out.shape[2]
    rows_of = lambda n: pl.BlockSpec((tile, n), lambda i, info: (i, 0))
    return pl.pallas_call(
        out_proj_kernel,
        grid_spec=pltpu.PrefetchScalarGridSpec(
            num_scalar_prefetch=1,
            grid=(tok // tile,),
            in_specs=[rows_of(width)]
            + [rows_of(feats)] * 4
            + [whole(w_out.shape), pl.BlockSpec((1, width), lambda i, info: (0, 0))],
            out_specs=[
                rows_of(width),
                rows_of(width),
                pl.BlockSpec((width, tile), lambda i, info: (0, i)),
                pl.BlockSpec((4, tile, feats), lambda i, info: (0, i, 0)),
            ],
        ),
        out_shape=[
            shape_of((tok, width), F32),
            shape_of((tok, width), BF16),
            shape_of((width, tok), BF16),
            shape_of((4, tok, feats), BF16),
        ],
        compiler_params=settings(1, 32),
        cost_estimate=cost(2 * tok * width * 4 * feats, 16 << 20),
        name="out_proj",
    )(info, x, *mine, *theirs, w_out, gain)


def norm_two_back_kernel(
    info, g_ref, r_ref, gr_ref, gain_ref, w_ref, gres_ref, gat_ref, a0, a1, b0, b1, gg_ref
):
    ctx = info[2]
    grad, resid = g_ref[...], r_ref[...]
    rho = lax.rsqrt(jnp.mean(resid * resid, axis=-1, keepdims=True) + EPS)
    unit = resid * rho
    scaled = grad * gain_ref[...]
    back = rho * (scaled - unit * jnp.mean(scaled * unit, axis=-1, keepdims=True))
    total = gr_ref[...] + back
    gres_ref[...] = total
    low = total.astype(BF16)
    gat_ref[...] = total.T.astype(BF16)

    @pl.when(pl.program_id(0) == 0)
    def _():
        gg_ref[...] = jnp.zeros_like(gg_ref)

    gg_ref[...] += jnp.sum(grad * unit, axis=0, keepdims=True)
    for j, ref, side in ((0, a0, ctx), (1, a1, ctx), (0, b0, 1 - ctx), (1, b1, 1 - ctx)):
        ref[...] = dot(low, w_ref[2 * side + j], 1, 0).astype(BF16)


def norm_two_back(info, grad, resid, grad_result, gain, w_out, tile):
    tok, width = grad.shape
    feats = w_out.shape[2]
    rows_of = lambda n: pl.BlockSpec((tile, n), lambda i, info: (i, 0))
    row = pl.BlockSpec((1, width), lambda i, info: (0, 0))
    return pl.pallas_call(
        norm_two_back_kernel,
        grid_spec=pltpu.PrefetchScalarGridSpec(
            num_scalar_prefetch=1,
            grid=(tok // tile,),
            in_specs=[rows_of(width)] * 3 + [row, whole(w_out.shape)],
            out_specs=[rows_of(width), pl.BlockSpec((width, tile), lambda i, info: (0, i))]
            + [rows_of(feats)] * 4
            + [row],
        ),
        out_shape=[shape_of((tok, width), F32), shape_of((width, tok), BF16)]
        + [shape_of((tok, feats), BF16)] * 4
        + [shape_of((1, width), F32)],
        compiler_params=settings(1, 32),
        cost_estimate=cost(2 * tok * width * 4 * feats, 24 << 20),
        name="norm_two_back",
    )(info, grad, resid, grad_result, gain, w_out)


def norm_one_back_kernel(info, p0, p1, w_ref, x_ref, gres_ref, gain_ref, out_ref, gg_ref):
    quarter = x_ref.shape[1] // 4
    grad = dot(p0[0], w_ref[0], 1, 1)
    grad = grad + dot(p1[0], w_ref[1], 1, 1)
    grad = grad + dot(p0[1], w_ref[2], 1, 1)
    grad = grad + dot(p1[1], w_ref[3], 1, 1)
    x = x_ref[...].astype(F32)
    rho = lax.rsqrt(jnp.mean(x * x, axis=-1, keepdims=True) + EPS)
    unit = x * rho
    scaled = grad * gain_ref[...]
    back = rho * (scaled - unit * jnp.mean(scaled * unit, axis=-1, keepdims=True))
    total = (gres_ref[...] + back).astype(BF16)
    for p, mask in enumerate(MASKS):
        at = pl.multiple_of(jnp.bitwise_xor(info[1], mask) * quarter, quarter)
        out_ref[:, pl.ds(at, quarter)] = total[:, p * quarter : (p + 1) * quarter]

    @pl.when(pl.program_id(0) == 0)
    def _():
        gg_ref[...] = jnp.zeros_like(gg_ref)

    gg_ref[...] += jnp.sum(grad * unit, axis=0, keepdims=True)


def norm_one_back(info, pairs, w_proj, x, grad_resid, gain, tile):
    tok, width = x.shape
    cols = w_proj.shape[2]
    rows_of = lambda n: pl.BlockSpec((tile, n), lambda i, info: (i, 0))
    pair = pl.BlockSpec((2, tile, cols), lambda i, info: (0, i, 0))
    row = pl.BlockSpec((1, width), lambda i, info: (0, 0))
    return pl.pallas_call(
        norm_one_back_kernel,
        grid_spec=pltpu.PrefetchScalarGridSpec(
            num_scalar_prefetch=1,
            grid=(tok // tile,),
            in_specs=[pair, pair, whole(w_proj.shape), rows_of(width), rows_of(width), row],
            out_specs=[rows_of(width), row],
        ),
        out_shape=[shape_of((tok, width), BF16), shape_of((1, width), F32)],
        compiler_params=settings(1, 32),
        cost_estimate=cost(2 * tok * width * 4 * cols, 18 << 20),
        name="norm_one_back",
    )(info, *pairs, w_proj, x, grad_resid, gain)


def weight_copies(plan, pieces, gate_up, down, gate_up_sem, down_sem):
    third = down.shape[1] // 3
    rows = down.shape[0] // 4
    wide, thin = [], []
    for p, chunks in enumerate(plan):
        block = pl.ds(p * rows, rows)
        for j, (piece, at) in enumerate(chunks):
            src = pieces[piece]
            wide.append(
                pltpu.make_async_copy(
                    src.at[:, pl.ds(at, 2 * third)],
                    gate_up.at[block, pl.ds(j * 2 * third, 2 * third)],
                    gate_up_sem,
                )
            )
            thin.append(
                pltpu.make_async_copy(
                    src.at[:, pl.ds(at + 2 * third, third)],
                    down.at[block, pl.ds(j * third, third)],
                    down_sem,
                )
            )
    return wide, thin


def split_act(act):
    third = act.shape[1] // 6
    part = lambda j: act[:, j * third : (j + 1) * third]
    return [(part(0), part(1)), (part(2), part(3)), (part(4), part(5))]


def ffn_fwd_kernel(
    tile,
    plans,
    info,
    scale,
    x_ref,
    resid_ref,
    teach_ref,
    *rest,
):
    pieces = []
    for plan in plans:
        count = 1 + max(piece for chunks in plan for piece, _ in chunks)
        pieces.append(rest[:count])
        rest = rest[count:]
    act_ref, hid_ref, out_ref, gres_ref, low_ref, lowt_ref, sq_ref = rest[:7]
    gate_up, down, total, sems = rest[7:]
    step, part = pl.program_id(0), pl.program_id(1)
    width = x_ref.shape[1]
    quarter = width // 4
    third = down.shape[2] // 3

    def copies(s):
        return weight_copies(
            plans[s], pieces[s], gate_up.at[s], down.at[s], sems.at[s, 0], sems.at[s, 1]
        )

    @pl.when((step == 0) & (part == 0))
    def _():
        for s in range(4):
            wide, thin = copies(s)
            for copy in wide + thin:
                copy.start()

    for s in range(4):

        @pl.when((step == s) & (part == 0))
        def _():
            pltpu.make_async_copy(gate_up.at[s], gate_up.at[s], sems.at[s, 0]).wait()
            pltpu.make_async_copy(down.at[s], down.at[s], sems.at[s, 1]).wait()

    rows = pl.ds(pl.multiple_of(part * tile, tile), tile)
    act = dot(x_ref[rows, :], gate_up[step], 1, 0)
    for j, (gate, upper) in enumerate(split_act(act)):
        hid_ref[0, :, j * third : (j + 1) * third] = (gate * sigmoid(gate) * upper).astype(BF16)
    act_ref[0] = act.astype(BF16)
    grown = dot(hid_ref[0], down[step], 1, 1)

    @pl.when(step == 0)
    def _():
        total[rows, :] = resid_ref[rows, :] + grown

    @pl.when((step > 0) & (step < 3))
    def _():
        total[rows, :] += grown

    @pl.when(step == 3)
    def _():
        result = total[rows, :] + grown
        total[rows, :] = result
        tok = x_ref.shape[0]
        slot = info[2] * tok + part * tile + lax.broadcasted_iota(jnp.int32, (tile, 1), 0)
        valid = jnp.where(slot < info[3], 1.0, 0.0)
        square = jnp.zeros((tile, quarter), F32)
        for p, mask in enumerate(MASKS):
            at = pl.multiple_of(jnp.bitwise_xor(info[1], mask) * quarter, quarter)
            cols = slice(p * quarter, (p + 1) * quarter)
            value = result[:, cols]
            out_ref[:, pl.ds(at, quarter)] = value.astype(BF16)
            error = valid * (value - teach_ref[0, :, pl.ds(at, quarter)].astype(F32))
            square = square + error * error
            grad = error * scale[0]
            gres_ref[:, cols] = grad
            low_ref[:, cols] = grad.astype(BF16)
            lowt_ref[cols, :] = grad.T.astype(BF16)

        @pl.when(part == 0)
        def _():
            sq_ref[...] = jnp.zeros_like(sq_ref)

        sq_ref[...] += jnp.sum(square, axis=0, keepdims=True)


def ffn_fwd(info, scale, x, resid, teacher, weights, units, tile):
    tok, width = x.shape
    pieces = [piece for _, group in weights for piece in group]
    last = lambda s, i: jnp.where(s == 3, i, 0)
    tiles = lambda n: pl.BlockSpec((tile, n), lambda s, i, info: (last(s, i), 0))
    return pl.pallas_call(
        functools.partial(ffn_fwd_kernel, tile, [plan for plan, _ in weights]),
        grid_spec=pltpu.PrefetchScalarGridSpec(
            num_scalar_prefetch=1,
            grid=(4, tok // tile),
            in_specs=[
                SMEM,
                whole((tok, width)),
                whole((tok, width)),
                pl.BlockSpec((1, tile, width), lambda s, i, info: (info[0], last(s, i), 0)),
            ]
            + [ANY] * len(pieces),
            out_specs=[
                pl.BlockSpec((1, tile, 2 * units), lambda s, i, info: (s, i, 0)),
                pl.BlockSpec((1, tile, units), lambda s, i, info: (s, i, 0)),
                tiles(width),
                tiles(width),
                tiles(width),
                pl.BlockSpec((width, tile), lambda s, i, info: (0, last(s, i))),
                pl.BlockSpec((1, width // 4), lambda s, i, info: (0, 0)),
            ],
            scratch_shapes=[
                pltpu.VMEM((4, width, 2 * units), BF16),
                pltpu.VMEM((4, width, units), BF16),
                pltpu.VMEM((tok, width), F32),
                pltpu.SemaphoreType.DMA((4, 2)),
            ],
        ),
        out_shape=[
            shape_of((4, tok, 2 * units), BF16),
            shape_of((4, tok, units), BF16),
            shape_of((tok, width), BF16),
            shape_of((tok, width), F32),
            shape_of((tok, width), BF16),
            shape_of((width, tok), BF16),
            shape_of((1, width // 4), F32),
        ],
        compiler_params=settings(2, 61),
        cost_estimate=cost(2 * tok * width * units * 12, 70 << 20),
        name="ffn_fwd",
    )(info, scale, x, resid, teacher, *pieces)


def ffn_bwd_kernel(steps, plan, first, low_ref, act_ref, hid_ref, xt_ref, lowt_ref, *rest):
    count = 1 + max(piece for chunks in plan for piece, _ in chunks)
    pieces, rest = rest[:count], rest[count:]
    if not first:
        in_ref, rest = rest[0], rest[1:]
    out_ref, keep_ref, send_ref, gate_up, down, dact_all, hid_all, sems = rest
    step = pl.program_id(0)
    units = down.shape[1]
    third = units // 3
    tile = low_ref.shape[0]

    @pl.when(step == 0)
    def _():
        wide, thin = weight_copies(plan, pieces, gate_up, down, sems.at[0], sems.at[1])
        for copy in thin + wide:
            copy.start()
        pltpu.make_async_copy(down, down, sems.at[1]).wait()

    @pl.when(step < steps)
    def _():
        rows = pl.ds(pl.multiple_of(step * tile, tile), tile)
        grad_hidden = dot(low_ref[...], down[...], 1, 0)
        for j, (gate, upper) in enumerate(split_act(act_ref[0])):
            grad = grad_hidden[:, j * third : (j + 1) * third]
            gate, upper = gate.astype(F32), upper.astype(F32)
            sig = sigmoid(gate)
            silu = gate * sig
            at = 2 * j * third
            dact_all[rows, at : at + third] = (
                grad * upper * (sig + silu - silu * sig)
            ).astype(BF16)
            dact_all[rows, at + third : at + 2 * third] = (grad * silu).astype(BF16)
        hid_all[rows, :] = hid_ref[0]

        @pl.when(step == 0)
        def _():
            pltpu.make_async_copy(gate_up, gate_up, sems.at[0]).wait()

        grown = dot(dact_all[rows, :], gate_up[...], 1, 1)
        out_ref[...] = grown if first else in_ref[...] + grown

    def weight_rows(target):
        target[:, : 2 * units] = dot(xt_ref[...], dact_all[...], 1, 0).astype(BF16)
        target[:, 2 * units :] = dot(lowt_ref[...], hid_all[...], 1, 0).astype(BF16)

    @pl.when((step >= steps) & (step < steps + 2))
    def _():
        weight_rows(send_ref)

    @pl.when(step >= steps + 2)
    def _():
        weight_rows(keep_ref)


def ffn_bwd(block, low, acts, hiddens, weights, total, xt, lowt, tile):
    plan, pieces = weights
    tok, width = low.shape
    units = hiddens.shape[2]
    steps = tok // tile
    quarter = width // 4
    first = total is None
    clip = lambda i: jnp.minimum(i, steps - 1)
    rows_of = lambda n: pl.BlockSpec((tile, n), lambda i: (clip(i), 0))
    slab = lambda n: pl.BlockSpec((1, tile, n), lambda i: (block, clip(i), 0))
    feature = lambda i: (jnp.where(i < steps + 2, jnp.maximum(i - steps, 0) + 2, i - steps - 2), 0)
    return pl.pallas_call(
        functools.partial(ffn_bwd_kernel, steps, plan, first),
        grid=(steps + 4,),
        in_specs=[
            rows_of(width),
            slab(2 * units),
            slab(units),
            pl.BlockSpec((quarter, tok), feature),
            pl.BlockSpec((quarter, tok), feature),
        ]
        + [ANY] * len(pieces)
        + ([] if first else [rows_of(width)]),
        out_specs=[
            rows_of(width),
            pl.BlockSpec((quarter, 3 * units), lambda i: (jnp.maximum(i - steps - 2, 0), 0)),
            pl.BlockSpec((quarter, 3 * units), lambda i: (jnp.clip(i - steps, 0, 1), 0)),
        ],
        out_shape=[
            shape_of((tok, width), F32),
            shape_of((width // 2, 3 * units), BF16),
            shape_of((width // 2, 3 * units), BF16),
        ],
        scratch_shapes=[
            pltpu.VMEM((width, 2 * units), BF16),
            pltpu.VMEM((width, units), BF16),
            pltpu.VMEM((tok, 2 * units), BF16),
            pltpu.VMEM((tok, units), BF16),
            pltpu.SemaphoreType.DMA((2,)),
        ],
        input_output_aliases={} if first else {5 + len(pieces): 0},
        compiler_params=settings(1, 56),
        cost_estimate=cost(2 * tok * width * units * 6, 32 << 20),
        name="ffn_bwd",
    )(low, acts, hiddens, xt, lowt, *pieces, *([] if first else [total]))


def after(value, *others):
    return lax.optimization_barrier((value,) + others)[0]


def z_gather(block):
    one = lax.ppermute(block, "tp", Z_UP)
    three = lax.ppermute(block, "tp", Z_DOWN)
    two = lax.ppermute(one, "tp", Z_UP)
    return [block, one, two, three]


def add(left, right):
    return left.astype(F32) + right.astype(F32)


def add_low(left, right):
    return add(left, right).astype(BF16)


def turn_chunks(block):
    wide = block.shape[1] * 2 // 9
    thin = wide // 2
    starts = [(2 * wide, wide), (wide, wide), (0, wide)]
    starts += [(3 * wide + 2 * thin, thin), (3 * wide + thin, thin), (3 * wide, thin)]
    return jnp.concatenate([block[:, a : a + n] for a, n in starts], axis=1)


def z_reduce(parts):
    two = add_low(parts[1], lax.ppermute(parts[2], "tp", Z_DOWN))
    total = add(parts[0], lax.ppermute(two, "tp", Z_DOWN))
    return total + lax.ppermute(parts[3], "tp", Z_UP).astype(F32)


def per_device_rows(
    tokens,
    teacher,
    lengths,
    attn_gain,
    q_weight,
    k_weight,
    v_weight,
    q_gain,
    k_gain,
    o_weight,
    ffn_gain,
    gate_weight,
    up_weight,
    down_weight,
):
    z = lax.axis_index("tp")
    ctx = lax.axis_index("ctx")
    fsdp = lax.axis_index("fsdp")
    rows_dev, tok, width = tokens.shape
    quarter = width // 4
    hd = q_gain.shape[0] * 4
    q_cols, k_cols = q_weight.shape[1], k_weight.shape[1]
    proj = q_cols + 2 * k_cols
    heads = (q_cols // hd, k_cols // hd)
    units = gate_weight.shape[1]
    slots = rows_dev * 4 * tok * 2

    def x_swap(v):
        return lax.ppermute(v, "fsdp", X_SWAP)

    def core_swap(v):
        return lax.ppermute(v, "fsdp", CORE_SWAP)

    def y_swap(v):
        return lax.ppermute(v, "ctx", Y_SWAP)

    length = lax.dynamic_slice_in_dim(lengths, z, 1, 0)
    info = jnp.concatenate([jnp.stack([z, fsdp, ctx]).astype(jnp.int32), length])

    w_attn, w_ffn = pack(
        info, q_weight, k_weight, v_weight, o_weight, gate_weight, up_weight, down_weight
    )
    count_here = jnp.sum(lengths).astype(F32)[None]
    vector = jnp.concatenate([attn_gain, ffn_gain, q_gain, k_gain]).astype(F32)
    vector = jnp.concatenate([vector, count_here, jnp.zeros((640 - 545,), F32)])[None]
    vector = jnp.concatenate([vector, x_swap(vector)], axis=0)
    vector = jnp.concatenate([vector, core_swap(vector)], axis=0)
    gain_one = vector[:, :quarter].reshape(1, width)
    gain_two = vector[:, quarter : 2 * quarter].reshape(1, width)
    total_count = jnp.sum(vector[:, 544])
    head_gains = vector[:, 2 * quarter : 544]
    head_gains = jnp.where(fsdp // 2 == 0, head_gains, head_gains[jnp.array([1, 0, 3, 2])])
    head_gains = jnp.where(fsdp % 2 == 0, head_gains, head_gains[jnp.array([2, 3, 0, 1])])
    head_gains = head_gains[jnp.array([0, 2, 1, 3])]
    gain_q = head_gains[:, : hd // 4].reshape(hd, 1)
    gain_k = head_gains[:, hd // 4 :].reshape(hd, 1)

    attn_blocks = [
        w_attn,
        lax.ppermute(w_attn, "tp", Z_UP),
        lax.ppermute(w_attn, "tp", Z_FAR),
        lax.ppermute(w_attn, "tp", Z_DOWN),
    ]
    attn_pieces = []
    for block in attn_blocks:
        far = x_swap(block)
        attn_pieces.append([block, far, core_swap(block), core_swap(far)])
    w_proj = jnp.concatenate([p[:, :proj] for b in attn_pieces for p in b], axis=0)
    w_proj = w_proj.reshape(4, width, proj)
    w_out = jnp.concatenate([p[:, proj:] for b in attn_pieces for p in b], axis=0)
    w_out = w_out.reshape(4, width, q_cols)

    ffn_one = lax.ppermute(after(w_ffn, attn_blocks[1]), "tp", Z_UP)
    ffn_three = lax.ppermute(after(w_ffn, attn_blocks[3]), "tp", Z_DOWN)
    ffn_two = [
        lax.ppermute(ffn_one[:, j * units : (j + 1) * units], "tp", Z_UP) for j in range(3)
    ]
    in_block = lambda i: [(i, 0), (i, units), (i, 2 * units)]
    in_pair = lambda i: [(i, 0), (i, units), (i + 1, 0)]
    plan_whole = [in_block(0), in_pair(1), in_block(3), in_pair(4)]
    plan_chunks = [[(3 * p + j, 0) for j in range(3)] for p in range(4)]

    def ffn_pieces(block, then):
        far = x_swap(block[:, : 2 * units])
        last = y_swap(after(far[:, :units], then))
        return [block, far, last, core_swap(block), core_swap(far), core_swap(last)]

    def ffn_chunks(blocks, then):
        far = [x_swap(blocks[0]), x_swap(blocks[1])]
        far.append(y_swap(after(far[0], then)))
        pieces = blocks + far
        return pieces + [core_swap(p) for p in pieces]

    x_in, normed_one_t = norm_one(info, tokens, gain_one, 256)
    pos = (ctx * tok + jnp.arange(tok, dtype=jnp.int32)).astype(F32)
    frequency = THETA ** (-(2.0 * jnp.arange(hd // 2, dtype=F32)) / hd)
    angles = frequency[:, None] * pos[None, :]
    tables = (jnp.cos(angles), jnp.sin(angles), gain_q, gain_k)

    def make(block):
        return project(info, w_proj, normed_one_t, *tables, heads, block)

    theirs = [make(lambda s: 2 * (1 - s[2])), make(lambda s: 2 * (1 - s[2]) + 1)]
    got = [y_swap(theirs[0][0]), y_swap(theirs[1][0])]
    mine = [make(lambda s: 2 * s[2]), make(lambda s: 2 * s[2] + 1)]

    outs = [attn_fwd(info, mine[j][0], got[j], hd) for j in range(2)]
    arrived = [y_swap(outs[j][1]) for j in range(2)]
    resid, normed_two, normed_two_t, attended = out_proj(
        info, x_in, [outs[0][0], outs[1][0]], arrived, w_out, gain_two, 256
    )

    own_ffn = after(w_ffn, attn_pieces[1][1], attn_pieces[3][1])
    ffn_weights = [
        (plan_whole, ffn_pieces(own_ffn, got[1])),
        (plan_whole, ffn_pieces(ffn_one, got[1])),
        (plan_chunks, ffn_chunks(ffn_two, outs[1][1])),
        (plan_whole, ffn_pieces(ffn_three, outs[0][1])),
    ]
    order = (0, 1, 3, 2)
    scale = (slots / total_count)[None]
    acts, hiddens, result_low, grad_result, grad_low, grad_low_t, square = ffn_fwd(
        info, scale, normed_two, resid, teacher, [ffn_weights[k] for k in order], units, 256
    )

    def spread(parts, dtype):
        out = jnp.zeros((rows_dev, tok, width), dtype)
        for k in (0, 1, 3, 2):
            part = parts[k].astype(dtype)[None]
            out = lax.dynamic_update_slice(out, part, (lax.rem(z - k + 4, 4), 0, 0))
        return out

    output_parts = z_gather(result_low)

    def halves(v):
        half = v.shape[0] // 2
        return (
            lax.dynamic_slice_in_dim(v, ctx * half, half, 0),
            lax.dynamic_slice_in_dim(v, half - ctx * half, half, 0),
        )

    def core_sum(keep, send):
        came = core_swap(send)
        return add_low(keep[:quarter], came[:quarter]), add_low(keep[quarter:], came[quarter:])

    def plane_sum(own, far, x_first, turn):
        if x_first:
            own = add_low(own, x_swap(far))
            here, there = halves(own)
            return add_low(here, turn(y_swap(there)))
        here, there = halves(own)
        far_here, far_there = halves(far)
        came = turn(y_swap(jnp.concatenate([there, far_there], axis=0)))
        half = quarter // 2
        return add_low(
            add_low(here, came[:half]), x_swap(add_low(far_here, came[half:]))
        )

    def finish(own, turn):
        other = turn(y_swap(own))
        return jnp.concatenate(
            [jnp.where(ctx == 0, own, other), jnp.where(ctx == 0, other, own)], axis=0
        )

    def ffn_back(k, total):
        return ffn_bwd(
            order.index(k),
            grad_low,
            acts,
            hiddens,
            ffn_weights[k],
            total,
            normed_two_t,
            grad_low_t,
            256,
        )

    def y_sum(own):
        here, there = halves(own)
        return add_low(here, turn_chunks(y_swap(there)))

    grad_two, keep2, send2 = ffn_back(2, None)
    grad_two, keep1, send1 = ffn_back(1, grad_two)
    own2, far2 = core_sum(keep2, send2)
    grad_two, keep3, send3 = ffn_back(3, after(grad_two, own2, far2))
    own1, far1 = core_sum(keep1, send1)
    grad_two, keep0, send0 = ffn_back(0, after(grad_two, own1, far1))
    own3, far3 = core_sum(keep3, send3)
    own2 = add_low(own2, x_swap(far2))
    grad_resid, grad_attn_t, a0, a1, b0, b1, gain_two_sum = norm_two_back(
        info, after(grad_two, own2, own3, far3), resid, grad_result, gain_two, w_out, 256
    )

    grad_got = [y_swap(b0), y_swap(b1)]
    own0, far0 = core_sum(keep0, send0)

    def attn_back(j, grad):
        return attn_bwd(
            info, mine[j][0], got[j], outs[j][0], outs[j][1], grad, grad_got[j], outs[j][2], hd
        )

    first_back = attn_back(0, after(a0, own0, far0))
    part2 = y_sum(after(own2, grad_got[1]))
    own1 = add_low(own1, x_swap(far1))
    second_back = attn_back(1, after(a1, first_back[1], own1, part2, output_parts[1]))
    part1 = y_sum(after(own1, first_back[1]))
    own3 = add_low(own3, x_swap(after(far3, own1)))
    output_parts[2] = after(output_parts[2], second_back[1])
    grad_heads = [y_swap(first_back[1]), y_swap(second_back[1])]
    two_down = add_low(part1, lax.ppermute(part2, "tp", Z_DOWN))
    back = [
        head_back(
            info,
            after(first_back[0], part1, own3),
            grad_heads[0],
            mine[0][1],
            theirs[0][1],
            *tables,
            heads,
        ),
        head_back(
            info, second_back[0], grad_heads[1], mine[1][1], theirs[1][1], *tables, heads
        ),
    ]
    part3 = y_sum(after(own3, grad_heads[1]))
    own0 = add_low(own0, x_swap(after(far0, own3)))
    part0 = y_sum(after(own0, part3))
    tokens_low, gain_one_sum = norm_one_back(
        info, [back[0][0], back[1][0]], w_proj, x_in, grad_resid, gain_one, 256
    )
    tokens_grad = spread(z_gather(tokens_low), F32)
    output = spread([after(part, tokens_low) for part in output_parts], BF16)

    attn_parts = []
    for k in range(4):
        part = jnp.concatenate(
            [
                dot(normed_one_t, back[k % 2][0][k // 2], 1, 0).astype(BF16),
                dot(grad_attn_t, attended[k], 1, 0).astype(BF16),
            ],
            axis=1,
        )
        own, far = core_sum(part[: width // 2], part[width // 2 :])
        attn_parts.append(plane_sum(own, far, k in (1, 2), lambda v: v))

    ffn_sum = add(part0, lax.ppermute(two_down, "tp", Z_DOWN))
    ffn_sum = ffn_sum + lax.ppermute(part3, "tp", Z_UP).astype(F32)
    ffn_grad = finish(ffn_sum, turn_chunks)
    attn_grad = finish(z_reduce(attn_parts), lambda v: v)

    def total(v):
        for axis, pairs in (("fsdp", CORE_SWAP), ("fsdp", X_SWAP), ("ctx", Y_SWAP)):
            v = v + lax.ppermute(v, axis, pairs)
        for pairs in (Z_NEAR, Z_FAR):
            v = v + lax.ppermute(v, "tp", pairs)
        return v

    def natural(v):
        v = v.reshape(4, quarter)[jnp.array([0, 2, 1, 3])]
        v = jnp.where(fsdp % 2 == 0, v, v[jnp.array([1, 0, 3, 2])])
        return jnp.where(fsdp // 2 == 0, v, v[jnp.array([2, 3, 0, 1])]).reshape(1, width)

    gain_heads = back[0][1] + back[1][1]
    sums = total(
        jnp.concatenate(
            [
                natural(gain_one_sum),
                natural(gain_two_sum),
                gain_heads[:, 0].reshape(1, hd),
                gain_heads[:, 1].reshape(1, hd),
                jnp.sum(square).reshape(1, 1),
                jnp.zeros((1, 127), F32),
            ],
            axis=1,
        )
    )[0]
    teacher_loss = sums[2 * width + 2 * hd] / (total_count * width)

    def own_part(at, size):
        return lax.dynamic_slice_in_dim(sums, at + fsdp * (size // 4), size // 4, 0)

    third = units // 3

    def columns(first):
        starts = [first(j) for j in range(3)]
        parts = [ffn_grad[:, s : s + third] for s in starts]
        return jnp.concatenate(
            [jnp.where(ctx == 0, parts[0], parts[2]), parts[1], jnp.where(ctx == 0, parts[2], parts[0])],
            axis=1,
        )

    return (
        output,
        teacher_loss,
        tokens_grad,
        own_part(0, width),
        attn_grad[:, :q_cols],
        attn_grad[:, q_cols : q_cols + k_cols],
        attn_grad[:, q_cols + k_cols : proj],
        own_part(2 * width, hd),
        own_part(2 * width + hd, hd),
        attn_grad[:, proj:].T,
        own_part(width, width),
        columns(lambda j: 2 * j * third),
        columns(lambda j: (2 * j + 1) * third),
        columns(lambda j: 2 * units + j * third).T,
    )


def solution(mesh):
    return jax.shard_map(
        per_device_rows if fits(mesh) else per_device_any,
        mesh=mesh,
        in_specs=(
            P("fsdp", "ctx", None),
            P("fsdp", "ctx", None),
            P("fsdp"),
            P("fsdp"),
            P("fsdp", "tp"),
            P("fsdp", "tp"),
            P("fsdp", "tp"),
            P("fsdp"),
            P("fsdp"),
            P("tp", "fsdp"),
            P("fsdp"),
            P("fsdp", "tp"),
            P("fsdp", "tp"),
            P("tp", "fsdp"),
        ),
        out_specs=(
            P("fsdp", "ctx", None),
            P(),
            P("fsdp", "ctx", None),
            P("fsdp"),
            P("fsdp", "tp"),
            P("fsdp", "tp"),
            P("fsdp", "tp"),
            P("fsdp"),
            P("fsdp"),
            P("tp", "fsdp"),
            P("fsdp"),
            P("fsdp", "tp"),
            P("fsdp", "tp"),
            P("tp", "fsdp"),
        ),
        check_vma=False,
    )
```

```python
import functools
import math

import jax
import jax.numpy as jnp
from jax import lax
from jax.experimental import pallas as pl
from jax.experimental.pallas import tpu as pltpu
from jax.sharding import PartitionSpec as P

EPS = 1e-05
THETA = 1000000.0
NEGATIVE = -1e30


def rms_scale(field_in, gain_vec):
    return (
        field_in * lax.rsqrt(jnp.mean(field_in * field_in, axis=-1, keepdims=True) + EPS) * gain_vec
    )


def rotate(field_in, positions):
    half_dim = field_in.shape[-1] // 2
    frequency = THETA ** (-(2.0 * jnp.arange(half_dim, dtype=jnp.float32)) / field_in.shape[-1])
    angles = positions[:, None] * frequency[None, :]
    cos_part = jnp.cos(angles)[:, None, :]
    sin_part = jnp.sin(angles)[:, None, :]
    lower_half = field_in[..., :half_dim]
    upper_half = field_in[..., half_dim:]
    return jnp.concatenate(
        [
            lower_half * cos_part - upper_half * sin_part,
            upper_half * cos_part + lower_half * sin_part,
        ],
        axis=-1,
    )


def linear(left_mat, right_mat):
    return jnp.dot(left_mat, right_mat, preferred_element_type=jnp.float32)


def linear_left(left_mat, right_mat):
    return lax.dot_general(
        left_mat, right_mat, (((0,), (0,)), ((), ())), preferred_element_type=jnp.float32
    )


def linear_right(left_mat, right_mat):
    return lax.dot_general(
        left_mat, right_mat, (((1,), (1,)), ((), ())), preferred_element_type=jnp.float32
    )


def swiglu(gate_act, up_act):
    return jax.nn.silu(gate_act) * up_act


def per_device_any(
    tokens,
    teacher,
    lengths,
    attn_gain,
    q_weight,
    k_weight,
    v_weight,
    q_gain,
    k_gain,
    o_weight,
    ffn_gain,
    gate_weight,
    up_weight,
    down_weight,
):
    (
        gain_one,
        w_query,
        w_key,
        w_value,
        gain_query,
        gain_key,
        w_output,
        gain_two,
        w_gate,
        w_upper,
        w_down,
    ) = (
        lax.all_gather(attn_gain, "fsdp", axis=0, tiled=True),
        lax.all_gather(q_weight, "fsdp", axis=0, tiled=True),
        lax.all_gather(k_weight, "fsdp", axis=0, tiled=True),
        lax.all_gather(v_weight, "fsdp", axis=0, tiled=True),
        lax.all_gather(q_gain, "fsdp", axis=0, tiled=True),
        lax.all_gather(k_gain, "fsdp", axis=0, tiled=True),
        lax.all_gather(o_weight, "fsdp", axis=1, tiled=True),
        lax.all_gather(ffn_gain, "fsdp", axis=0, tiled=True),
        lax.all_gather(gate_weight, "fsdp", axis=0, tiled=True),
        lax.all_gather(up_weight, "fsdp", axis=0, tiled=True),
        lax.all_gather(down_weight, "fsdp", axis=1, tiled=True),
    )
    rows_dev, block_len, model_width = tokens.shape
    count_tok = rows_dev * block_len
    head_dim = gain_query.shape[0]
    q_heads = w_query.shape[1] // head_dim
    kv_heads = w_key.shape[1] // head_dim
    group_size = q_heads // kv_heads
    score_scale = head_dim ** (-0.5)
    row_len = block_len * lax.axis_size("ctx")
    key_block = math.gcd(row_len, 512)
    block_start = lax.axis_index("ctx") * block_len
    tiles_used = (block_start + block_len + key_block - 1) // key_block
    slot_pos = block_start + jnp.arange(block_len, dtype=jnp.int32)
    positions = slot_pos.astype(jnp.float32)
    valid = (slot_pos[None, :] < lengths[:, None]).astype(jnp.float32)
    slots = count_tok * lax.axis_size("fsdp") * lax.axis_size("ctx")
    gain_two_f = gain_two.astype(jnp.float32)
    gain_one_f = gain_one.astype(jnp.float32)
    inputs = tokens.astype(jnp.float32)
    normed_one, back_one = jax.vjp(rms_scale, inputs, gain_one_f)
    normed_low = normed_one.astype(jnp.bfloat16).reshape(count_tok, model_width)
    query_raw = linear(normed_low, w_query)
    key_raw = linear(normed_low, w_key)
    value_raw = linear(normed_low, w_value)

    def heads_post(raw_heads, gain_vec):
        shaped = raw_heads.reshape(rows_dev, block_len, -1, head_dim)
        return rotate(rms_scale(shaped, gain_vec), positions)

    query_rot, query_back = jax.vjp(heads_post, query_raw, gain_query.astype(jnp.float32))
    key_rot, key_back = jax.vjp(heads_post, key_raw, gain_key.astype(jnp.float32))
    queries = query_rot.astype(jnp.bfloat16).reshape(
        rows_dev, block_len, kv_heads, group_size, head_dim
    )
    key_rows = key_rot.astype(jnp.bfloat16).reshape(rows_dev, block_len, kv_heads * head_dim)
    values = value_raw.astype(jnp.bfloat16).reshape(rows_dev, block_len, kv_heads * head_dim)
    keys_all, values_all = (
        lax.all_gather(key_rows, "ctx", axis=1, tiled=True),
        lax.all_gather(values, "ctx", axis=1, tiled=True),
    )

    def key_tile(tile_index):
        tile_start = tile_index * key_block
        key_pos = tile_start + jnp.arange(key_block, dtype=jnp.int32)
        key_part = lax.dynamic_slice_in_dim(keys_all, tile_start, key_block, 1).reshape(
            rows_dev, key_block, kv_heads, head_dim
        )
        value_part = lax.dynamic_slice_in_dim(values_all, tile_start, key_block, 1).reshape(
            rows_dev, key_block, kv_heads, head_dim
        )
        scores = (
            jnp.einsum("rqhgd,rkhd->rhgqk", queries, key_part, preferred_element_type=jnp.float32)
            * score_scale
        )
        allowed = (key_pos[None, None, :] <= slot_pos[None, :, None]) & (
            key_pos[None, None, :] < lengths[:, None, None]
        )
        return (tile_start, scores, allowed[:, None, None], key_part, value_part)

    stat_shape = (rows_dev, kv_heads, group_size, block_len)

    def stats_step(tile_index, carried):
        running_max, running_sum = carried
        tile_start, scores, allowed, key_part, value_part = key_tile(tile_index)
        masked = jnp.where(allowed, scores, NEGATIVE)
        new_max = jnp.maximum(running_max, jnp.max(masked, axis=-1))
        terms = jnp.where(allowed, jnp.exp(masked - new_max[..., None]), 0.0)
        return (new_max, running_sum * jnp.exp(running_max - new_max) + jnp.sum(terms, axis=-1))

    running_max, running_sum = lax.fori_loop(
        0,
        tiles_used,
        stats_step,
        (jnp.full(stat_shape, NEGATIVE, jnp.float32), jnp.zeros(stat_shape, jnp.float32)),
    )
    log_total = running_max + jnp.log(running_sum)
    out_shape = (rows_dev, block_len, kv_heads, group_size, head_dim)

    def value_step(tile_index, carried):
        rounded_out, exact_out = carried
        tile_start, scores, allowed, key_part, value_part = key_tile(tile_index)
        tile_probs = jnp.where(allowed, jnp.exp(scores - log_total[..., None]), 0.0)
        rounded_out = rounded_out + jnp.einsum(
            "rhgqk,rkhd->rqhgd",
            tile_probs.astype(jnp.bfloat16),
            value_part,
            preferred_element_type=jnp.float32,
        )
        exact_out = exact_out + jnp.einsum(
            "rhgqk,rkhd->rqhgd", tile_probs, value_part.astype(jnp.float32)
        )
        return (rounded_out, exact_out)

    rounded_out, exact_out = lax.fori_loop(
        0,
        tiles_used,
        value_step,
        (jnp.zeros(out_shape, jnp.float32), jnp.zeros(out_shape, jnp.float32)),
    )
    attended = rounded_out.astype(jnp.bfloat16).reshape(count_tok, q_heads * head_dim)
    attn_total = lax.psum(linear(attended, w_output), "tp")
    resid = inputs + attn_total.reshape(rows_dev, block_len, model_width)
    normed_two, back_two = jax.vjp(rms_scale, resid, gain_two_f)
    normed_second = normed_two.astype(jnp.bfloat16).reshape(count_tok, model_width)
    gate_act = linear(normed_second, w_gate)
    up_act = linear(normed_second, w_upper)
    hidden_full, back_glu = jax.vjp(swiglu, gate_act, up_act)
    hidden = hidden_full.astype(jnp.bfloat16)
    ffn_total = lax.psum(linear(hidden, w_down), "tp")
    result = resid + ffn_total.reshape(rows_dev, block_len, model_width)
    error_value = result - teacher.astype(jnp.float32)
    valid_col = valid[..., None]
    total_square, total_count = lax.psum(
        (jnp.sum(valid_col * error_value * error_value), jnp.sum(valid)), ("fsdp", "ctx")
    )
    teacher_loss = total_square / (total_count * model_width)
    grad_result = valid_col * error_value * (slots / total_count)
    grad_low = grad_result.astype(jnp.bfloat16).reshape(count_tok, model_width)
    grad_down = linear_left(hidden, grad_low)
    grad_hidden = linear_right(grad_low, w_down)
    grad_gate_full, grad_up_full = back_glu(grad_hidden)
    grad_gate = grad_gate_full.astype(jnp.bfloat16)
    grad_up = grad_up_full.astype(jnp.bfloat16)
    grad_wgate = linear_left(normed_second, grad_gate)
    grad_wup = linear_left(normed_second, grad_up)
    normed_two_part = linear_right(grad_gate, w_gate) + linear_right(grad_up, w_upper)
    grad_normed_two = lax.psum(normed_two_part, "tp")
    grad_resid_norm, grad_gain_two = back_two(
        grad_normed_two.reshape(rows_dev, block_len, model_width)
    )
    grad_resid = grad_result + grad_resid_norm
    grad_attn_low = grad_resid.astype(jnp.bfloat16).reshape(count_tok, model_width)
    grad_woutput = linear_left(attended, grad_attn_low)
    grad_attended = linear_right(grad_attn_low, w_output).astype(jnp.bfloat16).reshape(out_shape)
    delta = jnp.einsum("rqhgd,rqhgd->rhgq", grad_attended.astype(jnp.float32), exact_out)
    full_shape = (rows_dev, row_len, kv_heads * head_dim)

    def grad_step(tile_index, carried):
        grad_queries, grad_keys, grad_values = carried
        tile_start, scores, allowed, key_part, value_part = key_tile(tile_index)
        tile_probs = jnp.where(allowed, jnp.exp(scores - log_total[..., None]), 0.0)
        grad_probs = jnp.einsum(
            "rqhgd,rkhd->rhgqk", grad_attended, value_part, preferred_element_type=jnp.float32
        )
        grad_scores = (tile_probs * (grad_probs - delta[..., None])).astype(jnp.bfloat16)
        grad_queries = (
            grad_queries
            + jnp.einsum(
                "rhgqk,rkhd->rqhgd", grad_scores, key_part, preferred_element_type=jnp.float32
            )
            * score_scale
        )
        key_term = (
            jnp.einsum(
                "rhgqk,rqhgd->rkhd", grad_scores, queries, preferred_element_type=jnp.float32
            )
            * score_scale
        )
        value_term = jnp.einsum(
            "rhgqk,rqhgd->rkhd",
            tile_probs.astype(jnp.bfloat16),
            grad_attended,
            preferred_element_type=jnp.float32,
        )
        grad_keys = lax.dynamic_update_slice_in_dim(
            grad_keys, key_term.reshape(rows_dev, key_block, kv_heads * head_dim), tile_start, 1
        )
        grad_values = lax.dynamic_update_slice_in_dim(
            grad_values, value_term.reshape(rows_dev, key_block, kv_heads * head_dim), tile_start, 1
        )
        return (grad_queries, grad_keys, grad_values)

    grad_queries, grad_keys, grad_values = lax.fori_loop(
        0,
        tiles_used,
        grad_step,
        (
            jnp.zeros(out_shape, jnp.float32),
            jnp.zeros(full_shape, jnp.float32),
            jnp.zeros(full_shape, jnp.float32),
        ),
    )
    key_grad, value_grad = (
        lax.psum_scatter(grad_keys, "ctx", scatter_dimension=1, tiled=True),
        lax.psum_scatter(grad_values, "ctx", scatter_dimension=1, tiled=True),
    )
    grad_query_raw, grad_gain_query = query_back(
        grad_queries.reshape(rows_dev, block_len, q_heads, head_dim)
    )
    grad_key_raw, grad_gain_key = key_back(
        key_grad.reshape(rows_dev, block_len, kv_heads, head_dim)
    )
    query_low = grad_query_raw.astype(jnp.bfloat16)
    key_low = grad_key_raw.astype(jnp.bfloat16)
    value_low = value_grad.reshape(count_tok, kv_heads * head_dim).astype(jnp.bfloat16)
    grad_wquery = linear_left(normed_low, query_low)
    grad_wkey = linear_left(normed_low, key_low)
    grad_wvalue = linear_left(normed_low, value_low)
    normed_part = (
        linear_right(query_low, w_query)
        + linear_right(key_low, w_key)
        + linear_right(value_low, w_value)
    )
    grad_normed_one, grad_gain_query, grad_gain_key = lax.psum(
        (normed_part, grad_gain_query, grad_gain_key), "tp"
    )
    grad_input_norm, grad_gain_one = back_one(
        grad_normed_one.reshape(rows_dev, block_len, model_width)
    )
    tokens_grad = grad_resid + grad_input_norm
    partials = (
        grad_gain_one,
        grad_wquery,
        grad_wkey,
        grad_wvalue,
        grad_gain_query,
        grad_gain_key,
        grad_woutput,
        grad_gain_two,
        grad_wgate,
        grad_wup,
        grad_down,
    )
    pieces = (
        lax.psum_scatter(partials[0], ("fsdp", "ctx"), scatter_dimension=0, tiled=True),
        lax.psum_scatter(partials[1], ("fsdp", "ctx"), scatter_dimension=0, tiled=True),
        lax.psum_scatter(partials[2], ("fsdp", "ctx"), scatter_dimension=0, tiled=True),
        lax.psum_scatter(partials[3], ("fsdp", "ctx"), scatter_dimension=0, tiled=True),
        lax.psum_scatter(partials[4], ("fsdp", "ctx"), scatter_dimension=0, tiled=True),
        lax.psum_scatter(partials[5], ("fsdp", "ctx"), scatter_dimension=0, tiled=True),
        lax.psum_scatter(partials[6], ("fsdp", "ctx"), scatter_dimension=1, tiled=True),
        lax.psum_scatter(partials[7], ("fsdp", "ctx"), scatter_dimension=0, tiled=True),
        lax.psum_scatter(partials[8], ("fsdp", "ctx"), scatter_dimension=0, tiled=True),
        lax.psum_scatter(partials[9], ("fsdp", "ctx"), scatter_dimension=0, tiled=True),
        lax.psum_scatter(partials[10], ("fsdp", "ctx"), scatter_dimension=1, tiled=True),
    )
    summed = (
        lax.all_gather(pieces[0], "ctx", axis=0, tiled=True),
        lax.all_gather(pieces[1], "ctx", axis=0, tiled=True),
        lax.all_gather(pieces[2], "ctx", axis=0, tiled=True),
        lax.all_gather(pieces[3], "ctx", axis=0, tiled=True),
        lax.all_gather(pieces[4], "ctx", axis=0, tiled=True),
        lax.all_gather(pieces[5], "ctx", axis=0, tiled=True),
        lax.all_gather(pieces[6], "ctx", axis=1, tiled=True),
        lax.all_gather(pieces[7], "ctx", axis=0, tiled=True),
        lax.all_gather(pieces[8], "ctx", axis=0, tiled=True),
        lax.all_gather(pieces[9], "ctx", axis=0, tiled=True),
        lax.all_gather(pieces[10], "ctx", axis=1, tiled=True),
    )
    return (
        result.astype(jnp.bfloat16),
        teacher_loss,
        tokens_grad,
        summed[0],
        summed[1],
        summed[2],
        summed[3],
        summed[4],
        summed[5],
        summed[6],
        summed[7],
        summed[8],
        summed[9],
        summed[10],
    )


BF16 = jnp.bfloat16
F32 = jnp.float32
LOG2E = math.log2(math.e)
X_SWAP = [(0, 2), (2, 0), (1, 3), (3, 1)]
CORE_SWAP = [(0, 1), (1, 0), (2, 3), (3, 2)]
Y_SWAP = [(0, 1), (1, 0)]
Z_UP = [(0, 1), (1, 2), (2, 3), (3, 0)]
Z_DOWN = [(0, 3), (1, 0), (2, 1), (3, 2)]
Z_NEAR = [(0, 1), (1, 0), (2, 3), (3, 2)]
Z_FAR = [(0, 2), (2, 0), (1, 3), (3, 1)]
MASKS = (0, 2, 1, 3)
ANY = pl.BlockSpec(memory_space=pl.ANY)
SMEM = pl.BlockSpec(memory_space=pltpu.SMEM)


def fits(mesh):
    return dict(mesh.shape) == {"fsdp": 4, "ctx": 2, "tp": 4}


def dot(left, right, left_dim, right_dim):
    return lax.dot_general(
        left, right, (((left_dim,), (right_dim,)), ((), ())), preferred_element_type=F32
    )


def sigmoid(v):
    return 0.5 * jnp.tanh(0.5 * v) + 0.5


def whole(shape):
    zeros = (0,) * len(shape)
    return pl.BlockSpec(shape, lambda *_: zeros, pipeline_mode=pl.Buffered(1))


def settings(dims, mib):
    return pltpu.CompilerParams(
        dimension_semantics=("arbitrary",) * dims, vmem_limit_bytes=mib << 20
    )


def shape_of(shape, dtype):
    return jax.ShapeDtypeStruct(shape, dtype)


def cost(flops, bytes_accessed):
    return pl.CostEstimate(flops=flops >> 8, bytes_accessed=bytes_accessed >> 8, transcendentals=0)


def pack_kernel(info, o_in, g_in, u_in, d_in, out_ref, ffn_ref, o_ref, g_ref, u_ref, d_ref, sems):
    ctx = info[2]
    pairs = ((o_in, o_ref), (g_in, g_ref), (u_in, u_ref), (d_in, d_ref))
    copies = [pltpu.make_async_copy(a, b, sems.at[i]) for i, (a, b) in enumerate(pairs)]
    for copy in copies:
        copy.start()
    for copy in copies:
        copy.wait()
    out_ref[...] = o_ref[...].astype(F32).T.astype(BF16)
    third = g_ref.shape[1] // 3
    for j in range(3):
        at = pl.multiple_of(jnp.where(ctx == 0, j, 2 - j) * third, third)
        base = 3 * third * j
        ffn_ref[:, base : base + third] = g_ref[:, pl.ds(at, third)]
        ffn_ref[:, base + third : base + 2 * third] = u_ref[:, pl.ds(at, third)]
        down = d_ref[pl.ds(at, third), :].astype(F32).T.astype(BF16)
        ffn_ref[:, base + 2 * third : base + 3 * third] = down


def pack(info, o, g, u, d):
    rows = g.shape[0]
    return pl.pallas_call(
        pack_kernel,
        in_specs=[SMEM] + [ANY] * 4,
        out_specs=[pl.BlockSpec(memory_space=pltpu.VMEM)] * 2,
        out_shape=[shape_of((rows, o.shape[0]), BF16), shape_of((rows, 3 * g.shape[1]), BF16)],
        scratch_shapes=[pltpu.VMEM(a.shape, BF16) for a in (o, g, u, d)]
        + [pltpu.SemaphoreType.DMA((4,))],
        compiler_params=pltpu.CompilerParams(vmem_limit_bytes=24 << 20),
        cost_estimate=cost(0, 6 << 20),
        name="pack",
    )(info, o, g, u, d)


def norm_one_kernel(info, tok_ref, gain_ref, x_ref, nt_ref, x32):
    quarter = x_ref.shape[1] // 4
    for p, mask in enumerate(MASKS):
        at = pl.multiple_of(jnp.bitwise_xor(info[1], mask) * quarter, quarter)
        part = tok_ref[0, :, pl.ds(at, quarter)]
        x_ref[:, p * quarter : (p + 1) * quarter] = part
        x32[:, p * quarter : (p + 1) * quarter] = part.astype(F32)
    x = x32[...]
    rho = lax.rsqrt(jnp.mean(x * x, axis=-1, keepdims=True) + EPS)
    nt_ref[...] = (x * rho * gain_ref[...]).T.astype(BF16)


def norm_one(info, tokens, gain, tile):
    _, tok, width = tokens.shape
    return pl.pallas_call(
        norm_one_kernel,
        grid_spec=pltpu.PrefetchScalarGridSpec(
            num_scalar_prefetch=1,
            grid=(tok // tile,),
            in_specs=[
                pl.BlockSpec((1, tile, width), lambda i, info: (info[0], i, 0)),
                pl.BlockSpec((1, width), lambda i, info: (0, 0)),
            ],
            out_specs=[
                pl.BlockSpec((tile, width), lambda i, info: (i, 0)),
                pl.BlockSpec((width, tile), lambda i, info: (0, i)),
            ],
            scratch_shapes=[pltpu.VMEM((tile, width), F32)],
        ),
        out_shape=[shape_of((tok, width), BF16), shape_of((width, tok), BF16)],
        compiler_params=settings(1, 24),
        cost_estimate=cost(0, 6 << 20),
        name="norm_one",
    )(info, tokens, gain)


def proj_kernel(heads, block, info, *refs):
    pieces = [refs[4 * k : 4 * k + 4] for k in range(4)]
    nt_ref, cos_ref, sin_ref, qg_ref, kg_ref, rot_ref, raw_ref, w_ref, sem = refs[16:]
    rows = w_ref.shape[0] // 4

    @pl.when(pl.program_id(0) == 0)
    def _():
        for k in range(4):

            @pl.when(block(info) == k)
            def _():
                for p, piece in enumerate(pieces[k]):
                    pltpu.make_async_copy(piece, w_ref.at[pl.ds(p * rows, rows)], sem).start()

        pltpu.make_async_copy(w_ref, w_ref, sem).wait()

    hd = qg_ref.shape[0]
    half = hd // 2
    raw = dot(w_ref[...], nt_ref[...], 0, 0)
    cos_part, sin_part = cos_ref[...], sin_ref[...]
    heads_q, heads_k = heads
    raw_ref[...] = raw.astype(BF16)
    for h in range(heads_q + heads_k):
        v = raw[h * hd : (h + 1) * hd]
        rho = lax.rsqrt(jnp.mean(v * v, axis=0, keepdims=True) + EPS)
        v = v * rho * (qg_ref[...] if h < heads_q else kg_ref[...])
        a, b = v[:half], v[half:]
        rot_ref[h * hd : h * hd + half, :] = (a * cos_part - b * sin_part).astype(BF16)
        rot_ref[h * hd + half : (h + 1) * hd, :] = (b * cos_part + a * sin_part).astype(BF16)
    at = (heads_q + heads_k) * hd
    rot_ref[at:, :] = raw[at:].astype(BF16)


def project(info, pieces, normed_t, cos_part, sin_part, gain_q, gain_k, heads, block):
    width, tok = normed_t.shape
    cols = pieces[0][0].shape[1]
    tile = min(512, tok)
    const = lambda a: pl.BlockSpec(a.shape, lambda i, info: (0, 0))
    tab = lambda a: pl.BlockSpec((a.shape[0], tile), lambda i, info: (0, i))
    return pl.pallas_call(
        functools.partial(proj_kernel, heads, block),
        grid_spec=pltpu.PrefetchScalarGridSpec(
            num_scalar_prefetch=1,
            grid=(tok // tile,),
            in_specs=[ANY] * 16
            + [tab(normed_t), tab(cos_part), tab(sin_part), const(gain_q), const(gain_k)],
            out_specs=[pl.BlockSpec((cols, tile), lambda i, info: (0, i))] * 2,
            scratch_shapes=[pltpu.VMEM((width, cols), BF16), pltpu.SemaphoreType.DMA],
        ),
        out_shape=[shape_of((cols, tok), BF16), shape_of((cols, tok), BF16)],
        compiler_params=settings(1, 24),
        cost_estimate=cost(2 * width * cols * tok, 6 << 20),
        name="project",
    )(info, *[p for b in pieces for p in b], normed_t, cos_part, sin_part, gain_q, gain_k)


def head_back_kernel(
    heads, info, dm_ref, dt_ref, rm_ref, rt_ref, cos_ref, sin_ref, qg_ref, kg_ref, out_ref, gg_ref
):
    step, part = pl.program_id(0), pl.program_id(1)
    hd = qg_ref.shape[0]
    half = hd // 2
    heads_q, heads_k = heads
    cos_part, sin_part = cos_ref[...], sin_ref[...]
    tile = cos_part.shape[1]

    @pl.when((step == 0) & (part == 0))
    def _():
        gg_ref[...] = jnp.zeros_like(gg_ref)

    def work(d_ref, r_ref):
        gain_q = jnp.zeros((hd, 1), F32)
        gain_k = jnp.zeros((hd, 1), F32)
        done = []
        for h in range(heads_q + heads_k):
            is_q = h < heads_q
            g = d_ref[h * hd : (h + 1) * hd, :].astype(F32)
            raw = r_ref[h * hd : (h + 1) * hd, :].astype(F32)
            a, b = g[:half], g[half:]
            turned = jnp.concatenate(
                [a * cos_part + b * sin_part, b * cos_part - a * sin_part], axis=0
            )
            rho = lax.rsqrt(jnp.mean(raw * raw, axis=0, keepdims=True) + EPS)
            unit = raw * rho
            prod = turned * unit
            scaled = turned * (qg_ref[...] if is_q else kg_ref[...])
            mean = jnp.mean(scaled * unit, axis=0, keepdims=True)
            done.append(rho * (scaled - unit * mean))
            total = jnp.sum(prod, axis=1, keepdims=True)
            if is_q:
                gain_q = gain_q + total
            else:
                gain_k = gain_k + total
        done.append(d_ref[(heads_q + heads_k) * hd :, :].astype(F32))
        out_ref[0] = jnp.concatenate(done, axis=0).T.astype(BF16)
        lane = lax.broadcasted_iota(jnp.int32, gg_ref.shape, 1)
        gg_ref[...] += jnp.where(lane == 0, gain_q, jnp.where(lane == 1, gain_k, 0.0))

    @pl.when(step == 0)
    def _():
        work(dm_ref, rm_ref)

    @pl.when(step == 1)
    def _():
        work(dt_ref, rt_ref)


def head_back(info, grad_mine, grad_theirs, raw_mine, raw_theirs, cos_part, sin_part, gq, gk, heads):
    cols, tok = grad_mine.shape
    tile = min(512, tok)
    mine = pl.BlockSpec((cols, tile), lambda s, i, info: (0, jnp.where(s == 0, i, tok // tile - 1)))
    theirs = pl.BlockSpec((cols, tile), lambda s, i, info: (0, jnp.where(s == 0, 0, i)))
    tab = lambda a: pl.BlockSpec((a.shape[0], tile), lambda s, i, info: (0, i))
    const = lambda a: pl.BlockSpec(a.shape, lambda s, i, info: (0, 0))
    return pl.pallas_call(
        functools.partial(head_back_kernel, heads),
        grid_spec=pltpu.PrefetchScalarGridSpec(
            num_scalar_prefetch=1,
            grid=(2, tok // tile),
            in_specs=[
                mine,
                theirs,
                mine,
                theirs,
                tab(cos_part),
                tab(sin_part),
                const(gq),
                const(gk),
            ],
            out_specs=[
                pl.BlockSpec(
                    (1, tile, cols), lambda s, i, info: (jnp.bitwise_xor(info[2], s), i, 0)
                ),
                pl.BlockSpec((gq.shape[0], 128), lambda s, i, info: (0, 0)),
            ],
        ),
        out_shape=[shape_of((2, tok, cols), BF16), shape_of((gq.shape[0], 128), F32)],
        compiler_params=settings(2, 24),
        cost_estimate=cost(0, 8 << 20),
        name="head_back",
    )(info, grad_mine, grad_theirs, raw_mine, raw_theirs, cos_part, sin_part, gq, gk)


def load_rows(info, mine_ref, got_ref, rows, sems):
    tok = mine_ref.shape[1]
    ctx = info[2]
    here = pl.multiple_of(ctx * tok, tok)
    there = pl.multiple_of((1 - ctx) * tok, tok)
    one = pltpu.make_async_copy(mine_ref, rows.at[:, pl.ds(here, tok)], sems.at[0])
    two = pltpu.make_async_copy(got_ref, rows.at[:, pl.ds(there, tok)], sems.at[1])
    one.start()
    two.start()
    one.wait()
    two.wait()


def keys_with_bias(keys, length):
    hd, slots = keys.shape
    pos = lax.broadcasted_iota(jnp.int32, (hd, slots), 1)
    row = lax.broadcasted_iota(jnp.int32, (hd, slots), 0)
    bias = jnp.where((row == 0) & (pos >= length), NEGATIVE, 0.0)
    return jnp.concatenate([keys.astype(F32), bias], axis=0).T.astype(BF16)


def query_with_one(pair):
    one_row = jnp.where(lax.broadcasted_iota(jnp.int32, pair.shape, 0) == 0, 1.0, 0.0)
    return jnp.concatenate([pair, one_row.astype(BF16)], axis=0)


def causal(scores, width):
    key_pos = lax.broadcasted_iota(jnp.int32, (width, width), 0)
    query_pos = lax.broadcasted_iota(jnp.int32, (width, width), 1)
    allowed = key_pos <= query_pos
    return jnp.where(jnp.concatenate([allowed, allowed], axis=1), scores, NEGATIVE)


def attn_fwd_kernel(
    width, hd, info, mine_ref, got_ref, keep_ref, send_ref, lse_ref, rows, key_rows, sems
):
    head, block = pl.program_id(0), pl.program_id(1)
    heads_k = pl.num_programs(0)
    scale = hd**-0.5 * LOG2E
    length = info[3]
    key_at = pl.multiple_of(heads_k * 2 * hd + head * hd, hd)
    value_at = pl.multiple_of(heads_k * 3 * hd + head * hd, hd)
    query_at = pl.multiple_of(head * 2 * hd, 2 * hd)

    @pl.when((head == 0) & (block == 0))
    def _():
        load_rows(info, mine_ref, got_ref, rows, sems)

    @pl.when(block == 0)
    def _():
        key_rows[...] = keys_with_bias(rows[pl.ds(key_at, hd), :], length)

    start = pl.multiple_of(block * width, width)
    both = rows[pl.ds(query_at, 2 * hd), pl.ds(start, width)]
    query = query_with_one(jnp.concatenate([both[:hd], both[hd:]], axis=1))

    def tile(at, carried, diagonal):
        out, total = carried
        scores = dot(key_rows[pl.ds(at, width), :], query, 1, 0)
        if diagonal:
            scores = causal(scores, width)
        probs = jnp.exp2(scores * scale)
        total = total + jnp.sum(probs, axis=0, keepdims=True)
        out = out + dot(rows[pl.ds(value_at, hd), pl.ds(at, width)], probs.astype(BF16), 1, 0)
        return out, total

    carried = (jnp.zeros((hd, 2 * width), F32), jnp.zeros((1, 2 * width), F32))
    full = jnp.minimum(block, lax.div(length + width - 1, width))
    carried = lax.fori_loop(
        0, full, lambda j, c: tile(pl.multiple_of(j * width, width), c, False), carried
    )
    out, total = tile(start, carried, True)
    out = out * (1.0 / total)
    out = jnp.concatenate([out[:, :width], out[:, width:]], axis=0).T.astype(BF16)
    here = block // 2 == info[2]

    @pl.when(here)
    def _():
        keep_ref[...] = out

    @pl.when(jnp.logical_not(here))
    def _():
        send_ref[...] = out

    log_total = jnp.log2(total)
    lse_ref[0, 0:1, :] = log_total[:, :width]
    lse_ref[0, 1:2, :] = log_total[:, width:]


def keep_block(i, info):
    return jnp.clip(i - 2 * info[2], 0, 1)


def send_block(i, info):
    return jnp.clip(i - 2 * (1 - info[2]), 0, 1)


def attn_fwd(info, mine, got, hd):
    cols, tok = mine.shape
    heads_k = cols // (4 * hd)
    width = tok // 2
    return pl.pallas_call(
        functools.partial(attn_fwd_kernel, width, hd),
        grid_spec=pltpu.PrefetchScalarGridSpec(
            num_scalar_prefetch=1,
            grid=(heads_k, 4),
            in_specs=[ANY, ANY],
            out_specs=[
                pl.BlockSpec((width, 2 * hd), lambda h, i, info: (keep_block(i, info), h)),
                pl.BlockSpec((width, 2 * hd), lambda h, i, info: (send_block(i, info), h)),
                pl.BlockSpec((1, 2, width), lambda h, i, info: (h, 0, i)),
            ],
            scratch_shapes=[
                pltpu.VMEM((cols, 2 * tok), BF16),
                pltpu.VMEM((2 * tok, 2 * hd), BF16),
                pltpu.SemaphoreType.DMA((2,)),
            ],
        ),
        out_shape=[
            shape_of((tok, heads_k * 2 * hd), BF16),
            shape_of((tok, heads_k * 2 * hd), BF16),
            shape_of((heads_k, 2, 2 * tok), F32),
        ],
        compiler_params=settings(2, 32),
        cost_estimate=cost(heads_k * 2 * tok * 2 * tok * 256 * 4, 8 << 20),
        name="attn_fwd",
    )(info, mine, got)


def attn_bwd_kernel(
    width,
    hd,
    info,
    mine_ref,
    got_ref,
    ok_ref,
    os_ref,
    gk_ref,
    gs_ref,
    lse_ref,
    keep_ref,
    send_ref,
    rows,
    key_rows,
    value_rows,
    key_sum,
    value_sum,
    sems,
):
    head, block = pl.program_id(0), pl.program_id(1)
    heads_k = pl.num_programs(0)
    scale = hd**-0.5
    length = info[3]
    ctx = info[2]
    tok = keep_ref.shape[1]
    key_at = pl.multiple_of(heads_k * 2 * hd + head * hd, hd)
    value_at = pl.multiple_of(heads_k * 3 * hd + head * hd, hd)
    query_at = pl.multiple_of(head * 2 * hd, 2 * hd)

    @pl.when((head == 0) & (block == 0))
    def _():
        load_rows(info, mine_ref, got_ref, rows, sems)

    @pl.when(block == 0)
    def _():
        key_rows[...] = keys_with_bias(rows[pl.ds(key_at, hd), :], length)
        value_rows[...] = rows[pl.ds(value_at, hd), :].astype(F32).T.astype(BF16)
        key_sum[...] = jnp.zeros_like(key_sum)
        value_sum[...] = jnp.zeros_like(value_sum)

    start = pl.multiple_of(block * width, width)
    here = block // 2 == ctx

    def store_query(value):
        at = pl.ds(pl.multiple_of((block % 2) * width, width), width)

        @pl.when(here)
        def _():
            keep_ref[pl.ds(query_at, 2 * hd), at] = value

        @pl.when(jnp.logical_not(here))
        def _():
            send_ref[pl.ds(query_at, 2 * hd), at] = value

    @pl.when(block * width < length)
    def _():
        both = rows[pl.ds(query_at, 2 * hd), pl.ds(start, width)]
        pair = jnp.concatenate([both[:hd], both[hd:]], axis=1)
        query = query_with_one(pair)
        query_rows = pair.astype(F32).T.astype(BF16)
        grad_wide = jnp.where(here, gk_ref[...].astype(F32), gs_ref[...].astype(F32))
        out_wide = jnp.where(here, ok_ref[...].astype(F32), os_ref[...].astype(F32))
        grad_rows = jnp.concatenate([grad_wide[:, :hd], grad_wide[:, hd:]], axis=0).astype(BF16)
        grad_t = grad_wide.T
        prod = (grad_wide * out_wide).T
        grad = jnp.concatenate([grad_t[:hd], grad_t[hd:]], axis=1).astype(BF16)
        delta = jnp.concatenate(
            [
                jnp.sum(prod[:hd], axis=0, keepdims=True),
                jnp.sum(prod[hd:], axis=0, keepdims=True),
            ],
            axis=1,
        )
        lse = jnp.concatenate([lse_ref[0, 0:1, :], lse_ref[0, 1:2, :]], axis=1)

        def tile(at, query_sum, diagonal):
            scores = dot(key_rows[pl.ds(at, width), :], query, 1, 0)
            if diagonal:
                scores = causal(scores, width)
            probs = jnp.exp2(scores * (scale * LOG2E) - lse)
            grad_probs = dot(value_rows[pl.ds(at, width), :], grad, 1, 0)
            grad_scores = (probs * (grad_probs - delta)).astype(BF16)
            value_sum[pl.ds(at, width), :] += dot(probs.astype(BF16), grad_rows, 1, 0)
            key_sum[pl.ds(at, width), :] += dot(grad_scores, query_rows, 1, 0)
            return query_sum + dot(rows[pl.ds(key_at, hd), pl.ds(at, width)], grad_scores, 1, 0)

        query_sum = lax.fori_loop(
            0,
            block,
            lambda j, s: tile(pl.multiple_of(j * width, width), s, False),
            jnp.zeros((hd, 2 * width), F32),
        )
        query_sum = tile(start, query_sum, True) * scale
        store_query(
            jnp.concatenate([query_sum[:, :width], query_sum[:, width:]], axis=0).astype(BF16)
        )

    @pl.when(block * width >= length)
    def _():
        store_query(jnp.zeros((2 * hd, width), BF16))

    @pl.when(block == 3)
    def _():
        for at, total in ((key_at, key_sum[...] * scale), (value_at, value_sum[...])):
            total = total.T.astype(BF16)
            left, right = total[:, :tok], total[:, tok:]

            @pl.when(ctx == 0)
            def _():
                keep_ref[pl.ds(at, hd), :] = left
                send_ref[pl.ds(at, hd), :] = right

            @pl.when(ctx == 1)
            def _():
                keep_ref[pl.ds(at, hd), :] = right
                send_ref[pl.ds(at, hd), :] = left


def attn_bwd(info, mine, got, out_keep, out_send, grad_keep, grad_send, lse, hd):
    cols, tok = mine.shape
    heads_k = cols // (4 * hd)
    width = tok // 2
    keep = pl.BlockSpec((width, 2 * hd), lambda h, i, info: (keep_block(i, info), h))
    send = pl.BlockSpec((width, 2 * hd), lambda h, i, info: (send_block(i, info), h))
    full = pl.BlockSpec((cols, tok), lambda h, i, info: (0, 0))
    return pl.pallas_call(
        functools.partial(attn_bwd_kernel, width, hd),
        grid_spec=pltpu.PrefetchScalarGridSpec(
            num_scalar_prefetch=1,
            grid=(heads_k, 4),
            in_specs=[
                ANY,
                ANY,
                keep,
                send,
                keep,
                send,
                pl.BlockSpec((1, 2, width), lambda h, i, info: (h, 0, i)),
            ],
            out_specs=[full, full],
            scratch_shapes=[
                pltpu.VMEM((cols, 2 * tok), BF16),
                pltpu.VMEM((2 * tok, 2 * hd), BF16),
                pltpu.VMEM((2 * tok, hd), BF16),
                pltpu.VMEM((2 * tok, hd), F32),
                pltpu.VMEM((2 * tok, hd), F32),
                pltpu.SemaphoreType.DMA((2,)),
            ],
        ),
        out_shape=[shape_of((cols, tok), BF16), shape_of((cols, tok), BF16)],
        compiler_params=settings(2, 40),
        cost_estimate=cost(heads_k * 5 * tok * 2 * tok * 256 * 4, 12 << 20),
        name="attn_bwd",
    )(info, mine, got, out_keep, out_send, grad_keep, grad_send, lse)


def load_blocks(pieces, target, sem):
    rows = target.shape[1] // 4

    @pl.when(pl.program_id(0) == 0)
    def _():
        for i, piece in enumerate(pieces):
            block = target.at[i // 4, pl.ds(i % 4 * rows, rows)]
            pltpu.make_async_copy(piece, block, sem).start()
        pltpu.make_async_copy(target, target, sem).wait()


def out_proj_kernel(info, *refs):
    x_ref, a0, a1, b0, b1, gain_ref, r_ref, n_ref, nt_ref, att_ref, w_ref, sem = refs[16:]
    load_blocks(refs[:16], w_ref, sem)
    ctx = info[2]
    total = x_ref[...].astype(F32)
    for j, ref, side in ((0, a0, ctx), (1, a1, ctx), (0, b0, 1 - ctx), (1, b1, 1 - ctx)):
        block = 2 * side + j
        part = ref[...]
        att_ref[block] = part
        total = total + dot(part, w_ref[block], 1, 1)
    rho = lax.rsqrt(jnp.mean(total * total, axis=-1, keepdims=True) + EPS)
    normed = total * rho * gain_ref[...]
    r_ref[...] = total
    n_ref[...] = normed.astype(BF16)
    nt_ref[...] = normed.T.astype(BF16)


def out_proj(info, x, mine, theirs, pieces, gain, tile):
    tok, width = x.shape
    feats = pieces[0][0].shape[1]
    rows_of = lambda n: pl.BlockSpec((tile, n), lambda i, info: (i, 0))
    return pl.pallas_call(
        out_proj_kernel,
        grid_spec=pltpu.PrefetchScalarGridSpec(
            num_scalar_prefetch=1,
            grid=(tok // tile,),
            in_specs=[ANY] * 16
            + [rows_of(width)]
            + [rows_of(feats)] * 4
            + [pl.BlockSpec((1, width), lambda i, info: (0, 0))],
            out_specs=[
                rows_of(width),
                rows_of(width),
                pl.BlockSpec((width, tile), lambda i, info: (0, i)),
                pl.BlockSpec((4, tile, feats), lambda i, info: (0, i, 0)),
            ],
            scratch_shapes=[pltpu.VMEM((4, width, feats), BF16), pltpu.SemaphoreType.DMA],
        ),
        out_shape=[
            shape_of((tok, width), F32),
            shape_of((tok, width), BF16),
            shape_of((width, tok), BF16),
            shape_of((4, tok, feats), BF16),
        ],
        compiler_params=settings(1, 32),
        cost_estimate=cost(2 * tok * width * 4 * feats, 16 << 20),
        name="out_proj",
    )(info, *[p for b in pieces for p in b], x, *mine, *theirs, gain)


def norm_two_back_kernel(info, *refs):
    g_ref, r_ref, gr_ref, gain_ref, gres_ref, gat_ref, a0, a1, b0, b1, gg_ref, w_ref, sem = refs[16:]
    load_blocks(refs[:16], w_ref, sem)
    ctx = info[2]
    grad, resid = g_ref[...], r_ref[...]
    rho = lax.rsqrt(jnp.mean(resid * resid, axis=-1, keepdims=True) + EPS)
    unit = resid * rho
    scaled = grad * gain_ref[...]
    back = rho * (scaled - unit * jnp.mean(scaled * unit, axis=-1, keepdims=True))
    total = gr_ref[...] + back
    gres_ref[...] = total
    low = total.astype(BF16)
    gat_ref[...] = total.T.astype(BF16)

    @pl.when(pl.program_id(0) == 0)
    def _():
        gg_ref[...] = jnp.zeros_like(gg_ref)

    gg_ref[...] += jnp.sum(grad * unit, axis=0, keepdims=True)
    for j, ref, side in ((0, a0, ctx), (1, a1, ctx), (0, b0, 1 - ctx), (1, b1, 1 - ctx)):
        ref[...] = dot(low, w_ref[2 * side + j], 1, 0).astype(BF16)


def norm_two_back(info, grad, resid, grad_result, gain, pieces, tile):
    tok, width = grad.shape
    feats = pieces[0][0].shape[1]
    rows_of = lambda n: pl.BlockSpec((tile, n), lambda i, info: (i, 0))
    row = pl.BlockSpec((1, width), lambda i, info: (0, 0))
    return pl.pallas_call(
        norm_two_back_kernel,
        grid_spec=pltpu.PrefetchScalarGridSpec(
            num_scalar_prefetch=1,
            grid=(tok // tile,),
            in_specs=[ANY] * 16 + [rows_of(width)] * 3 + [row],
            out_specs=[rows_of(width), pl.BlockSpec((width, tile), lambda i, info: (0, i))]
            + [rows_of(feats)] * 4
            + [row],
            scratch_shapes=[pltpu.VMEM((4, width, feats), BF16), pltpu.SemaphoreType.DMA],
        ),
        out_shape=[shape_of((tok, width), F32), shape_of((width, tok), BF16)]
        + [shape_of((tok, feats), BF16)] * 4
        + [shape_of((1, width), F32)],
        compiler_params=settings(1, 32),
        cost_estimate=cost(2 * tok * width * 4 * feats, 24 << 20),
        name="norm_two_back",
    )(info, *[p for b in pieces for p in b], grad, resid, grad_result, gain)


def norm_one_back_kernel(info, *refs):
    p0, p1, x_ref, gres_ref, gain_ref, out_ref, gg_ref, w_ref, sem = refs[16:]
    load_blocks(refs[:16], w_ref, sem)
    quarter = x_ref.shape[1] // 4
    grad = dot(p0[0], w_ref[0], 1, 1)
    grad = grad + dot(p1[0], w_ref[1], 1, 1)
    grad = grad + dot(p0[1], w_ref[2], 1, 1)
    grad = grad + dot(p1[1], w_ref[3], 1, 1)
    x = x_ref[...].astype(F32)
    rho = lax.rsqrt(jnp.mean(x * x, axis=-1, keepdims=True) + EPS)
    unit = x * rho
    scaled = grad * gain_ref[...]
    back = rho * (scaled - unit * jnp.mean(scaled * unit, axis=-1, keepdims=True))
    total = (gres_ref[...] + back).astype(BF16)
    for p, mask in enumerate(MASKS):
        at = pl.multiple_of(jnp.bitwise_xor(info[1], mask) * quarter, quarter)
        out_ref[:, pl.ds(at, quarter)] = total[:, p * quarter : (p + 1) * quarter]

    @pl.when(pl.program_id(0) == 0)
    def _():
        gg_ref[...] = jnp.zeros_like(gg_ref)

    gg_ref[...] += jnp.sum(grad * unit, axis=0, keepdims=True)


def norm_one_back(info, pairs, pieces, x, grad_resid, gain, tile):
    tok, width = x.shape
    cols = pieces[0][0].shape[1]
    rows_of = lambda n: pl.BlockSpec((tile, n), lambda i, info: (i, 0))
    pair = pl.BlockSpec((2, tile, cols), lambda i, info: (0, i, 0))
    row = pl.BlockSpec((1, width), lambda i, info: (0, 0))
    return pl.pallas_call(
        norm_one_back_kernel,
        grid_spec=pltpu.PrefetchScalarGridSpec(
            num_scalar_prefetch=1,
            grid=(tok // tile,),
            in_specs=[ANY] * 16 + [pair, pair, rows_of(width), rows_of(width), row],
            out_specs=[rows_of(width), row],
            scratch_shapes=[pltpu.VMEM((4, width, cols), BF16), pltpu.SemaphoreType.DMA],
        ),
        out_shape=[shape_of((tok, width), BF16), shape_of((1, width), F32)],
        compiler_params=settings(1, 32),
        cost_estimate=cost(2 * tok * width * 4 * cols, 18 << 20),
        name="norm_one_back",
    )(info, *[p for b in pieces for p in b], *pairs, x, grad_resid, gain)


def weight_copies(plan, pieces, gate_up, down, gate_up_sem, down_sem):
    third = down.shape[1] // 3
    rows = down.shape[0] // 4
    wide, thin = [], []
    for p, chunks in enumerate(plan):
        block = pl.ds(p * rows, rows)
        for j, (piece, at) in enumerate(chunks):
            src = pieces[piece]
            wide.append(
                pltpu.make_async_copy(
                    src.at[:, pl.ds(at, 2 * third)],
                    gate_up.at[block, pl.ds(j * 2 * third, 2 * third)],
                    gate_up_sem,
                )
            )
            thin.append(
                pltpu.make_async_copy(
                    src.at[:, pl.ds(at + 2 * third, third)],
                    down.at[block, pl.ds(j * third, third)],
                    down_sem,
                )
            )
    return wide, thin


def split_act(act):
    third = act.shape[1] // 6
    part = lambda j: act[:, j * third : (j + 1) * third]
    return [(part(0), part(1)), (part(2), part(3)), (part(4), part(5))]


def ffn_fwd_kernel(tile, plans, last, info, scale, x_ref, in_ref, *rest):
    if last:
        teach_ref, rest = rest[0], rest[1:]
    pieces = []
    for plan in plans:
        count = 1 + max(piece for chunks in plan for piece, _ in chunks)
        pieces.append(rest[:count])
        rest = rest[count:]
    act_ref, hid_ref = rest[:2]
    if last:
        out_ref, gres_ref, low_ref, lowt_ref, sq_ref = rest[2:7]
        gate_up, down, total, sems = rest[7:]
    else:
        sum_ref, gate_up, down, total, sems = rest[2:]
    step, part = pl.program_id(0), pl.program_id(1)
    final = len(plans) - 1
    width = x_ref.shape[1]
    quarter = width // 4
    third = down.shape[2] // 3

    def copies(s):
        return weight_copies(
            plans[s], pieces[s], gate_up.at[s], down.at[s], sems.at[s, 0], sems.at[s, 1]
        )

    @pl.when((step == 0) & (part == 0))
    def _():
        for s in range(len(plans)):
            wide, thin = copies(s)
            for copy in wide + thin:
                copy.start()

    for s in range(len(plans)):

        @pl.when((step == s) & (part == 0))
        def _():
            pltpu.make_async_copy(gate_up.at[s], gate_up.at[s], sems.at[s, 0]).wait()
            pltpu.make_async_copy(down.at[s], down.at[s], sems.at[s, 1]).wait()

    rows = pl.ds(pl.multiple_of(part * tile, tile), tile)
    act = dot(x_ref[rows, :], gate_up[step], 1, 0)
    for j, (gate, upper) in enumerate(split_act(act)):
        hid_ref[0, :, j * third : (j + 1) * third] = (gate * sigmoid(gate) * upper).astype(BF16)
    act_ref[0] = act.astype(BF16)
    grown = dot(hid_ref[0], down[step], 1, 1)

    @pl.when(step == 0)
    def _():
        total[rows, :] = in_ref[...] + grown

    @pl.when(step > 0)
    def _():
        total[rows, :] += grown

    @pl.when(step == final)
    def _():
        result = total[rows, :]
        if not last:
            sum_ref[...] = result
            return
        tok = x_ref.shape[0]
        slot = info[2] * tok + part * tile + lax.broadcasted_iota(jnp.int32, (tile, 1), 0)
        valid = jnp.where(slot < info[3], 1.0, 0.0)
        square = jnp.zeros((tile, quarter), F32)
        for p, mask in enumerate(MASKS):
            at = pl.multiple_of(jnp.bitwise_xor(info[1], mask) * quarter, quarter)
            cols = slice(p * quarter, (p + 1) * quarter)
            value = result[:, cols]
            out_ref[:, pl.ds(at, quarter)] = value.astype(BF16)
            error = valid * (value - teach_ref[0, :, pl.ds(at, quarter)].astype(F32))
            square = square + error * error
            grad = error * scale[0]
            gres_ref[:, cols] = grad
            low_ref[:, cols] = grad.astype(BF16)
            lowt_ref[cols, :] = grad.T.astype(BF16)

        @pl.when(part == 0)
        def _():
            sq_ref[...] = jnp.zeros_like(sq_ref)

        sq_ref[...] += jnp.sum(square, axis=0, keepdims=True)


def ffn_fwd(info, scale, x, total, teacher, weights, units, tile):
    tok, width = x.shape
    pieces = [piece for _, group in weights for piece in group]
    count = len(weights)
    last = teacher is not None
    entry = lambda s, i: jnp.where(s == 0, i, tok // tile - 1)
    leave = lambda s, i: jnp.where(s == count - 1, i, 0)
    tiles = lambda n: pl.BlockSpec((tile, n), lambda s, i, info: (leave(s, i), 0))
    slab = lambda n: pl.BlockSpec((1, tile, n), lambda s, i, info: (s, i, 0))
    in_specs = [
        SMEM,
        whole((tok, width)),
        pl.BlockSpec((tile, width), lambda s, i, info: (entry(s, i), 0)),
    ]
    out_specs = [slab(2 * units), slab(units)]
    out_shape = [shape_of((count, tok, 2 * units), BF16), shape_of((count, tok, units), BF16)]
    if last:
        in_specs.append(
            pl.BlockSpec((1, tile, width), lambda s, i, info: (info[0], leave(s, i), 0))
        )
        out_specs += [
            tiles(width),
            tiles(width),
            tiles(width),
            pl.BlockSpec((width, tile), lambda s, i, info: (0, leave(s, i))),
            pl.BlockSpec((1, width // 4), lambda s, i, info: (0, 0)),
        ]
        out_shape += [
            shape_of((tok, width), BF16),
            shape_of((tok, width), F32),
            shape_of((tok, width), BF16),
            shape_of((width, tok), BF16),
            shape_of((1, width // 4), F32),
        ]
    else:
        out_specs.append(tiles(width))
        out_shape.append(shape_of((tok, width), F32))
    return pl.pallas_call(
        functools.partial(ffn_fwd_kernel, tile, [plan for plan, _ in weights], last),
        grid_spec=pltpu.PrefetchScalarGridSpec(
            num_scalar_prefetch=1,
            grid=(count, tok // tile),
            in_specs=in_specs + [ANY] * len(pieces),
            out_specs=out_specs,
            scratch_shapes=[
                pltpu.VMEM((count, width, 2 * units), BF16),
                pltpu.VMEM((count, width, units), BF16),
                pltpu.VMEM((tok, width), F32),
                pltpu.SemaphoreType.DMA((count, 2)),
            ],
        ),
        out_shape=out_shape,
        compiler_params=settings(2, 50),
        cost_estimate=cost(2 * tok * width * units * 3 * count, 20 << 20),
        name="ffn_fwd",
    )(info, scale, x, total, *([teacher] if last else []), *pieces)


def ffn_bwd_kernel(steps, plan, first, low_ref, act_ref, hid_ref, xt_ref, lowt_ref, *rest):
    count = 1 + max(piece for chunks in plan for piece, _ in chunks)
    pieces, rest = rest[:count], rest[count:]
    if not first:
        in_ref, rest = rest[0], rest[1:]
    out_ref, keep_ref, send_ref, gate_up, down, dact_all, hid_all, sems = rest
    step = pl.program_id(0)
    units = down.shape[1]
    third = units // 3
    tile = low_ref.shape[0]

    @pl.when(step == 0)
    def _():
        wide, thin = weight_copies(plan, pieces, gate_up, down, sems.at[0], sems.at[1])
        for copy in thin + wide:
            copy.start()
        pltpu.make_async_copy(down, down, sems.at[1]).wait()

    @pl.when(step < steps)
    def _():
        rows = pl.ds(pl.multiple_of(step * tile, tile), tile)
        grad_hidden = dot(low_ref[...], down[...], 1, 0)
        for j, (gate, upper) in enumerate(split_act(act_ref[0])):
            grad = grad_hidden[:, j * third : (j + 1) * third]
            gate, upper = gate.astype(F32), upper.astype(F32)
            sig = sigmoid(gate)
            silu = gate * sig
            at = 2 * j * third
            dact_all[rows, at : at + third] = (
                grad * upper * (sig + silu - silu * sig)
            ).astype(BF16)
            dact_all[rows, at + third : at + 2 * third] = (grad * silu).astype(BF16)
        hid_all[rows, :] = hid_ref[0]

        @pl.when(step == 0)
        def _():
            pltpu.make_async_copy(gate_up, gate_up, sems.at[0]).wait()

        grown = dot(dact_all[rows, :], gate_up[...], 1, 1)
        out_ref[...] = grown if first else in_ref[...] + grown

    def weight_rows(target):
        target[:, : 2 * units] = dot(xt_ref[...], dact_all[...], 1, 0).astype(BF16)
        target[:, 2 * units :] = dot(lowt_ref[...], hid_all[...], 1, 0).astype(BF16)

    @pl.when((step >= steps) & (step < steps + 2))
    def _():
        weight_rows(send_ref)

    @pl.when(step >= steps + 2)
    def _():
        weight_rows(keep_ref)


def ffn_bwd(low, saved, weights, total, xt, lowt, tile):
    plan, pieces = weights
    acts, hiddens, block = saved
    tok, width = low.shape
    units = hiddens.shape[2]
    steps = tok // tile
    quarter = width // 4
    first = total is None
    clip = lambda i: jnp.minimum(i, steps - 1)
    rows_of = lambda n: pl.BlockSpec((tile, n), lambda i: (clip(i), 0))
    slab = lambda n: pl.BlockSpec((1, tile, n), lambda i: (block, clip(i), 0))
    feature = lambda i: (jnp.where(i < steps + 2, jnp.maximum(i - steps, 0) + 2, i - steps - 2), 0)
    return pl.pallas_call(
        functools.partial(ffn_bwd_kernel, steps, plan, first),
        grid=(steps + 4,),
        in_specs=[
            rows_of(width),
            slab(2 * units),
            slab(units),
            pl.BlockSpec((quarter, tok), feature),
            pl.BlockSpec((quarter, tok), feature),
        ]
        + [ANY] * len(pieces)
        + ([] if first else [rows_of(width)]),
        out_specs=[
            rows_of(width),
            pl.BlockSpec((quarter, 3 * units), lambda i: (jnp.maximum(i - steps - 2, 0), 0)),
            pl.BlockSpec((quarter, 3 * units), lambda i: (jnp.clip(i - steps, 0, 1), 0)),
        ],
        out_shape=[
            shape_of((tok, width), F32),
            shape_of((width // 2, 3 * units), BF16),
            shape_of((width // 2, 3 * units), BF16),
        ],
        scratch_shapes=[
            pltpu.VMEM((width, 2 * units), BF16),
            pltpu.VMEM((width, units), BF16),
            pltpu.VMEM((tok, 2 * units), BF16),
            pltpu.VMEM((tok, units), BF16),
            pltpu.SemaphoreType.DMA((2,)),
        ],
        input_output_aliases={} if first else {5 + len(pieces): 0},
        compiler_params=settings(1, 56),
        cost_estimate=cost(2 * tok * width * units * 6, 32 << 20),
        name="ffn_bwd",
    )(low, acts, hiddens, xt, lowt, *pieces, *([] if first else [total]))


def turn_chunks(block):
    wide = block.shape[1] * 2 // 9
    thin = wide // 2
    starts = [(2 * wide, wide), (wide, wide), (0, wide)]
    starts += [(3 * wide + 2 * thin, thin), (3 * wide + thin, thin), (3 * wide, thin)]
    return jnp.concatenate([block[:, a : a + n] for a, n in starts], axis=1)


def sum_kernel(side, turn, info, left_ref, right_ref, *outs):
    right = right_ref[...]
    if turn:
        right = turn_chunks(right)
    total = (left_ref[...].astype(F32) + right.astype(F32)).astype(BF16)
    if len(outs) == 1:
        outs[0][...] = total
        return
    first = side(pl.program_id(0), info) == 0

    @pl.when(first)
    def _():
        outs[0][...] = total

    @pl.when(jnp.logical_not(first))
    def _():
        outs[1][...] = total


def summed(info, left, right, how, turn=False):
    rows, cols = left.shape
    count = rows // 128
    block = lambda at: pl.BlockSpec((128, cols), at)
    if how == "all":
        side, places = None, [lambda i, info: (i, 0)]
    elif how == "halves":
        half = count // 2
        side = lambda i, info: i // half
        places = [
            lambda i, info: (jnp.minimum(i, half - 1), 0),
            lambda i, info: (jnp.maximum(i - half, 0), 0),
        ]
    else:
        side = lambda i, info: jnp.bitwise_xor(i % 2, info[2])
        places = [lambda i, info: (i // 2, 0)] * 2
    shapes = [shape_of((rows // len(places), cols), BF16)] * len(places)
    out = pl.pallas_call(
        functools.partial(sum_kernel, side, turn),
        grid_spec=pltpu.PrefetchScalarGridSpec(
            num_scalar_prefetch=1,
            grid=(count,),
            in_specs=[block(lambda i, info: (i, 0))] * 2,
            out_specs=[block(at) for at in places],
        ),
        out_shape=shapes,
        compiler_params=settings(1, 24),
        cost_estimate=cost(0, 4 << 20),
        name="summed",
    )(info, left, right)
    return out[0] if len(places) == 1 else out


def after(value, *others):
    return lax.optimization_barrier((value,) + others)[0]


def z_gather(block):
    one = lax.ppermute(block, "tp", Z_UP)
    three = lax.ppermute(block, "tp", Z_DOWN)
    two = lax.ppermute(one, "tp", Z_UP)
    return [block, one, two, three]


def add(left, right):
    return left.astype(F32) + right.astype(F32)


def add_low(left, right):
    return add(left, right).astype(BF16)


def z_reduce(parts):
    two = add_low(parts[1], lax.ppermute(parts[2], "tp", Z_DOWN))
    total = add(parts[0], lax.ppermute(two, "tp", Z_DOWN))
    return total + lax.ppermute(parts[3], "tp", Z_UP).astype(F32)


def per_device_rows(
    tokens,
    teacher,
    lengths,
    attn_gain,
    q_weight,
    k_weight,
    v_weight,
    q_gain,
    k_gain,
    o_weight,
    ffn_gain,
    gate_weight,
    up_weight,
    down_weight,
):
    z = lax.axis_index("tp")
    ctx = lax.axis_index("ctx")
    fsdp = lax.axis_index("fsdp")
    rows_dev, tok, width = tokens.shape
    quarter = width // 4
    hd = q_gain.shape[0] * 4
    q_cols, k_cols = q_weight.shape[1], k_weight.shape[1]
    proj = q_cols + 2 * k_cols
    heads = (q_cols // hd, k_cols // hd)
    units = gate_weight.shape[1]
    slots = rows_dev * 4 * tok * 2

    def x_swap(v):
        return lax.ppermute(v, "fsdp", X_SWAP)

    def core_swap(v):
        return lax.ppermute(v, "fsdp", CORE_SWAP)

    def y_swap(v):
        return lax.ppermute(v, "ctx", Y_SWAP)

    length = lax.dynamic_slice_in_dim(lengths, z, 1, 0)
    info = jnp.concatenate([jnp.stack([z, fsdp, ctx]).astype(jnp.int32), length])

    w_proj = jnp.concatenate([q_weight, k_weight, v_weight], axis=1)
    w_out, w_ffn = pack(info, o_weight, gate_weight, up_weight, down_weight)
    count_here = jnp.sum(lengths).astype(F32)[None]
    vector = jnp.concatenate([attn_gain, ffn_gain, q_gain, k_gain]).astype(F32)
    vector = jnp.concatenate([vector, count_here, jnp.zeros((640 - 545,), F32)])[None]
    vector = jnp.concatenate([vector, x_swap(vector)], axis=0)
    vector = jnp.concatenate([vector, core_swap(vector)], axis=0)
    gain_one = vector[:, :quarter].reshape(1, width)
    gain_two = vector[:, quarter : 2 * quarter].reshape(1, width)
    total_count = jnp.sum(vector[:, 544])

    def natural(v):
        v = jnp.concatenate([v[0:1], v[2:3], v[1:2], v[3:4]], axis=0)
        v = jnp.where(fsdp % 2 == 0, v, jnp.concatenate([v[1:2], v[0:1], v[3:4], v[2:3]], axis=0))
        return jnp.where(fsdp // 2 == 0, v, jnp.concatenate([v[2:4], v[0:2]], axis=0))

    head_gains = natural(vector[:, 2 * quarter : 544])
    gain_q = head_gains[:, : hd // 4].reshape(hd, 1)
    gain_k = head_gains[:, hd // 4 :].reshape(hd, 1)

    def z_direct(block):
        return [
            block,
            lax.ppermute(block, "tp", Z_UP),
            lax.ppermute(block, "tp", Z_FAR),
            lax.ppermute(block, "tp", Z_DOWN),
        ]

    def plane_pieces(blocks):
        pieces = []
        for block in blocks:
            far = x_swap(block)
            pieces.append([block, far, core_swap(block), core_swap(far)])
        return pieces

    proj_blocks = z_direct(w_proj)
    proj_pieces = plane_pieces(proj_blocks)
    out_pieces = plane_pieces(z_direct(after(w_out, *proj_blocks[1:])))
    ffn_one = lax.ppermute(after(w_ffn, *proj_blocks[1:]), "tp", Z_UP)
    in_block = lambda i: [(i, 0), (i, units), (i, 2 * units)]
    in_pair = lambda i: [(i, 0), (i, units), (i + 1, 0)]
    plan_whole = [in_block(0), in_pair(1), in_block(3), in_pair(4)]
    plan_chunks = [[(3 * p + j, 0) for j in range(3)] for p in range(4)]

    def ffn_pieces(block, far, last):
        return plan_whole, [block, far, last, core_swap(block), core_swap(far), core_swap(last)]

    x_in, normed_one_t = norm_one(info, tokens, gain_one, 256)
    pos = (ctx * tok + jnp.arange(tok, dtype=jnp.int32)).astype(F32)
    frequency = THETA ** (-(2.0 * jnp.arange(hd // 2, dtype=F32)) / hd)
    angles = frequency[:, None] * pos[None, :]
    tables = (jnp.cos(angles), jnp.sin(angles), gain_q, gain_k)

    def make(block):
        return project(info, proj_pieces, normed_one_t, *tables, heads, block)

    far_of = lambda block: x_swap(block[:, : 2 * units])
    near = lambda far: far[:, :units]
    own_ffn = after(w_ffn, *[b[1] for b in proj_pieces])
    far0 = far_of(own_ffn)
    weights0 = ffn_pieces(own_ffn, far0, y_swap(near(far0)))

    theirs = [make(lambda s: 2 * (1 - s[2])), make(lambda s: 2 * (1 - s[2]) + 1)]
    got = [y_swap(theirs[0][0]), y_swap(theirs[1][0])]
    mine = [make(lambda s: 2 * s[2]), make(lambda s: 2 * s[2] + 1)]

    ffn_one = after(ffn_one, mine[1][0])
    far1 = far_of(ffn_one)
    ffn_three = lax.ppermute(after(w_ffn, ffn_one, mine[1][0]), "tp", Z_DOWN)
    first = attn_fwd(info, after(mine[0][0], far0), got[0], hd)
    second = attn_fwd(info, after(mine[1][0], first[1]), got[1], hd)
    outs = [first, second]
    arrived = [y_swap(first[1]), y_swap(second[1])]
    ffn_three = after(ffn_three, second[1])
    far3 = far_of(ffn_three)
    ffn_one, far1 = after(ffn_one, second[1]), after(far1, second[1])
    ffn_two = [
        lax.ppermute(after(ffn_one[:, j * units : (j + 1) * units], ffn_three), "tp", Z_UP)
        for j in range(3)
    ]
    last1 = y_swap(after(near(far1), arrived[1]))
    resid, normed_two, normed_two_t, attended = out_proj(
        info, x_in, [first[0], second[0]], arrived, out_pieces, gain_two, 256
    )

    scale = (slots / total_count)[None]
    weights1 = ffn_pieces(ffn_one, far1, after(last1, normed_two))
    two_first, two_middle = after(ffn_two[0], normed_two), after(ffn_two[1], normed_two)
    two_far = [x_swap(two_first), x_swap(two_middle)]
    far3 = after(far3, normed_two)
    last3 = y_swap(near(far3))
    acts_a, hiddens_a, sum_a = ffn_fwd(
        info, scale, normed_two, resid, None, [weights0, weights1], units, 256
    )
    weights3 = ffn_pieces(ffn_three, far3, after(last3, sum_a))
    two_far = [after(two_far[0], sum_a), after(two_far[1], sum_a)]
    two_far.append(y_swap(two_far[0]))
    acts_b, hiddens_b, sum_b = ffn_fwd(
        info, scale, normed_two, sum_a, None, [weights3], units, 256
    )
    two = [two_first, two_middle, after(ffn_two[2], sum_a)] + two_far[:2] + [after(two_far[2], sum_b)]
    weights2 = (plan_chunks, two + [core_swap(p) for p in two])
    acts_c, hiddens_c, result_low, grad_result, grad_low, grad_low_t, square = ffn_fwd(
        info, scale, normed_two, sum_b, teacher, [weights2], units, 256
    )

    def spread(parts, dtype):
        out = jnp.zeros((rows_dev, tok, width), dtype)
        for k in (0, 1, 3, 2):
            part = parts[k].astype(dtype)[None]
            out = lax.dynamic_update_slice(out, part, (lax.rem(z - k + 4, 4), 0, 0))
        return out

    def ffn_back(weights, saved, total):
        return ffn_bwd(
            grad_low, saved, weights, total, normed_two_t, grad_low_t, 256
        )

    output_one = lax.ppermute(result_low, "tp", Z_UP)
    total, keep2, send2 = ffn_back(weights2, (acts_c, hiddens_c, 0), None)
    came2 = core_swap(send2)
    total, keep1, send1 = ffn_back(weights1, (acts_a, hiddens_a, 1), after(total, send2))
    came1 = core_swap(send1)
    own2, far2 = summed(info, after(keep2, send1), came2, "halves")
    came2 = x_swap(far2)
    output_one = after(output_one, own2)
    output_three = lax.ppermute(after(result_low, output_one), "tp", Z_DOWN)
    total, keep3, send3 = ffn_back(weights3, (acts_b, hiddens_b, 0), after(total, own2, output_one))
    came3 = core_swap(send3)
    here1, there1 = summed(info, after(keep1, send3), came1, "ctx")
    came1 = y_swap(there1)
    total, keep0, send0 = ffn_back(weights0, (acts_a, hiddens_a, 0), after(total, here1))
    came0 = core_swap(send0)
    own3, far3 = summed(info, after(keep3, send0), came3, "halves")
    came3 = x_swap(far3)
    here2, there2 = summed(info, after(own2, own3), came2, "ctx")
    output_three = after(output_three, here2)
    output_two = lax.ppermute(after(output_one, output_three), "tp", Z_UP)
    grad_resid, grad_attn_t, a0, a1, b0, b1, gain_two_sum = norm_two_back(
        info, after(total, here2, output_three), resid, grad_result, gain_two, out_pieces, 256
    )

    grad_got = [y_swap(b0), y_swap(b1)]
    own0, far0 = summed(info, after(keep0, b0), came0, "halves")
    own1, far1 = summed(info, after(here1, own0), came1, "halves", True)
    came1 = x_swap(far1)
    came2 = y_swap(after(there2, grad_got[0]))

    def attn_back(j, grad):
        return attn_bwd(
            info, mine[j][0], got[j], outs[j][0], outs[j][1], grad, grad_got[j], outs[j][2], hd
        )

    first_back = attn_back(0, after(a0, own1))
    grad_heads = [y_swap(first_back[1])]
    part2 = summed(info, after(here2, first_back[1]), came2, "all", True)
    part1 = summed(info, after(own1, part2), came1, "all")
    here3, there3 = summed(info, after(own3, part1), came3, "ctx")
    came0 = x_swap(after(far0, here3))
    output_two = after(output_two, here3)
    came2 = lax.ppermute(after(part2, output_two), "tp", Z_DOWN)
    came3 = y_swap(after(there3, first_back[1]))
    second_back = attn_back(1, after(a1, here3, output_two))
    grad_heads.append(y_swap(second_back[1]))
    two_down = summed(info, after(part1, second_back[1]), came2, "all")
    came2 = lax.ppermute(two_down, "tp", Z_DOWN)
    back = [
        head_back(
            info,
            after(first_back[0], two_down),
            grad_heads[0],
            mine[0][1],
            theirs[0][1],
            *tables,
            heads,
        )
    ]
    part3 = summed(info, after(here3, back[0][0]), came3, "all", True)
    came3 = lax.ppermute(part3, "tp", Z_UP)
    back.append(
        head_back(
            info,
            after(second_back[0], part3),
            grad_heads[1],
            mine[1][1],
            theirs[1][1],
            *tables,
            heads,
        )
    )
    tokens_low, gain_one_sum = norm_one_back(
        info, [back[0][0], back[1][0]], proj_pieces, x_in, grad_resid, gain_one, 256
    )
    tokens_grad = spread(z_gather(tokens_low), F32)
    output_parts = [result_low, output_one, output_two, output_three]
    output = spread([after(part, tokens_low) for part in output_parts], BF16)

    def halves(v):
        half = v.shape[0] // 2
        return (
            lax.dynamic_slice_in_dim(v, ctx * half, half, 0),
            lax.dynamic_slice_in_dim(v, half - ctx * half, half, 0),
        )

    attn_parts = []
    for k in range(4):
        part = jnp.concatenate(
            [
                dot(normed_one_t, back[k % 2][0][k // 2], 1, 0).astype(BF16),
                dot(grad_attn_t, attended[k], 1, 0).astype(BF16),
            ],
            axis=1,
        )
        came = core_swap(part[width // 2 :])
        own = add_low(part[:quarter], came[:quarter])
        far = add_low(part[quarter : width // 2], came[quarter:])
        here, there = halves(add_low(own, x_swap(far)))
        attn_parts.append(add_low(here, y_swap(there)))

    here0, there0 = summed(info, after(own0, tokens_low), came0, "ctx")
    part0 = summed(info, here0, y_swap(there0), "all", True)

    def finish(own, turn):
        other = turn(y_swap(own))
        return jnp.concatenate(
            [jnp.where(ctx == 0, own, other), jnp.where(ctx == 0, other, own)], axis=0
        )

    ffn_sum = add(part0, came2) + came3.astype(F32)
    ffn_grad = finish(ffn_sum, turn_chunks)
    attn_grad = finish(z_reduce(attn_parts), lambda v: v)

    def total(v):
        for axis, pairs in (("fsdp", CORE_SWAP), ("fsdp", X_SWAP), ("ctx", Y_SWAP)):
            v = v + lax.ppermute(v, axis, pairs)
        for pairs in (Z_NEAR, Z_FAR):
            v = v + lax.ppermute(v, "tp", pairs)
        return v

    gain_heads = back[0][1] + back[1][1]
    sums = total(
        jnp.concatenate(
            [
                natural(gain_one_sum.reshape(4, quarter)).reshape(1, width),
                natural(gain_two_sum.reshape(4, quarter)).reshape(1, width),
                gain_heads[:, 0].reshape(1, hd),
                gain_heads[:, 1].reshape(1, hd),
                jnp.sum(square).reshape(1, 1),
                jnp.zeros((1, 127), F32),
            ],
            axis=1,
        )
    )[0]
    teacher_loss = sums[2 * width + 2 * hd] / (total_count * width)

    def own_part(at, size):
        return lax.dynamic_slice_in_dim(sums, at + fsdp * (size // 4), size // 4, 0)

    third = units // 3

    def columns(first):
        starts = [first(j) for j in range(3)]
        parts = [ffn_grad[:, s : s + third] for s in starts]
        return jnp.concatenate(
            [jnp.where(ctx == 0, parts[0], parts[2]), parts[1], jnp.where(ctx == 0, parts[2], parts[0])],
            axis=1,
        )

    return (
        output,
        teacher_loss,
        tokens_grad,
        own_part(0, width),
        attn_grad[:, :q_cols],
        attn_grad[:, q_cols : q_cols + k_cols],
        attn_grad[:, q_cols + k_cols : proj],
        own_part(2 * width, hd),
        own_part(2 * width + hd, hd),
        attn_grad[:, proj:].T,
        own_part(width, width),
        columns(lambda j: 2 * j * third),
        columns(lambda j: (2 * j + 1) * third),
        columns(lambda j: 2 * units + j * third).T,
    )


def solution(mesh):
    return jax.shard_map(
        per_device_rows if fits(mesh) else per_device_any,
        mesh=mesh,
        in_specs=(
            P("fsdp", "ctx", None),
            P("fsdp", "ctx", None),
            P("fsdp"),
            P("fsdp"),
            P("fsdp", "tp"),
            P("fsdp", "tp"),
            P("fsdp", "tp"),
            P("fsdp"),
            P("fsdp"),
            P("tp", "fsdp"),
            P("fsdp"),
            P("fsdp", "tp"),
            P("fsdp", "tp"),
            P("tp", "fsdp"),
        ),
        out_specs=(
            P("fsdp", "ctx", None),
            P(),
            P("fsdp", "ctx", None),
            P("fsdp"),
            P("fsdp", "tp"),
            P("fsdp", "tp"),
            P("fsdp", "tp"),
            P("fsdp"),
            P("fsdp"),
            P("tp", "fsdp"),
            P("fsdp"),
            P("fsdp", "tp"),
            P("fsdp", "tp"),
            P("tp", "fsdp"),
        ),
        check_vma=False,
    )
```

```python
import functools
import math

import jax
import jax.numpy as jnp
from jax import lax
from jax.experimental import pallas as pl
from jax.experimental.pallas import tpu as pltpu
from jax.sharding import PartitionSpec as P

EPS = 1e-05
THETA = 1000000.0
NEGATIVE = -1e30


def rms_scale(field_in, gain_vec):
    return (
        field_in * lax.rsqrt(jnp.mean(field_in * field_in, axis=-1, keepdims=True) + EPS) * gain_vec
    )


def rotate(field_in, positions):
    half_dim = field_in.shape[-1] // 2
    frequency = THETA ** (-(2.0 * jnp.arange(half_dim, dtype=jnp.float32)) / field_in.shape[-1])
    angles = positions[:, None] * frequency[None, :]
    cos_part = jnp.cos(angles)[:, None, :]
    sin_part = jnp.sin(angles)[:, None, :]
    lower_half = field_in[..., :half_dim]
    upper_half = field_in[..., half_dim:]
    return jnp.concatenate(
        [
            lower_half * cos_part - upper_half * sin_part,
            upper_half * cos_part + lower_half * sin_part,
        ],
        axis=-1,
    )


def linear(left_mat, right_mat):
    return jnp.dot(left_mat, right_mat, preferred_element_type=jnp.float32)


def linear_left(left_mat, right_mat):
    return lax.dot_general(
        left_mat, right_mat, (((0,), (0,)), ((), ())), preferred_element_type=jnp.float32
    )


def linear_right(left_mat, right_mat):
    return lax.dot_general(
        left_mat, right_mat, (((1,), (1,)), ((), ())), preferred_element_type=jnp.float32
    )


def swiglu(gate_act, up_act):
    return jax.nn.silu(gate_act) * up_act


def per_device_any(
    tokens,
    teacher,
    lengths,
    attn_gain,
    q_weight,
    k_weight,
    v_weight,
    q_gain,
    k_gain,
    o_weight,
    ffn_gain,
    gate_weight,
    up_weight,
    down_weight,
):
    (
        gain_one,
        w_query,
        w_key,
        w_value,
        gain_query,
        gain_key,
        w_output,
        gain_two,
        w_gate,
        w_upper,
        w_down,
    ) = (
        lax.all_gather(attn_gain, "fsdp", axis=0, tiled=True),
        lax.all_gather(q_weight, "fsdp", axis=0, tiled=True),
        lax.all_gather(k_weight, "fsdp", axis=0, tiled=True),
        lax.all_gather(v_weight, "fsdp", axis=0, tiled=True),
        lax.all_gather(q_gain, "fsdp", axis=0, tiled=True),
        lax.all_gather(k_gain, "fsdp", axis=0, tiled=True),
        lax.all_gather(o_weight, "fsdp", axis=1, tiled=True),
        lax.all_gather(ffn_gain, "fsdp", axis=0, tiled=True),
        lax.all_gather(gate_weight, "fsdp", axis=0, tiled=True),
        lax.all_gather(up_weight, "fsdp", axis=0, tiled=True),
        lax.all_gather(down_weight, "fsdp", axis=1, tiled=True),
    )
    rows_dev, block_len, model_width = tokens.shape
    count_tok = rows_dev * block_len
    head_dim = gain_query.shape[0]
    q_heads = w_query.shape[1] // head_dim
    kv_heads = w_key.shape[1] // head_dim
    group_size = q_heads // kv_heads
    score_scale = head_dim ** (-0.5)
    row_len = block_len * lax.axis_size("ctx")
    key_block = math.gcd(row_len, 512)
    block_start = lax.axis_index("ctx") * block_len
    tiles_used = (block_start + block_len + key_block - 1) // key_block
    slot_pos = block_start + jnp.arange(block_len, dtype=jnp.int32)
    positions = slot_pos.astype(jnp.float32)
    valid = (slot_pos[None, :] < lengths[:, None]).astype(jnp.float32)
    slots = count_tok * lax.axis_size("fsdp") * lax.axis_size("ctx")
    gain_two_f = gain_two.astype(jnp.float32)
    gain_one_f = gain_one.astype(jnp.float32)
    inputs = tokens.astype(jnp.float32)
    normed_one, back_one = jax.vjp(rms_scale, inputs, gain_one_f)
    normed_low = normed_one.astype(jnp.bfloat16).reshape(count_tok, model_width)
    query_raw = linear(normed_low, w_query)
    key_raw = linear(normed_low, w_key)
    value_raw = linear(normed_low, w_value)

    def heads_post(raw_heads, gain_vec):
        shaped = raw_heads.reshape(rows_dev, block_len, -1, head_dim)
        return rotate(rms_scale(shaped, gain_vec), positions)

    query_rot, query_back = jax.vjp(heads_post, query_raw, gain_query.astype(jnp.float32))
    key_rot, key_back = jax.vjp(heads_post, key_raw, gain_key.astype(jnp.float32))
    queries = query_rot.astype(jnp.bfloat16).reshape(
        rows_dev, block_len, kv_heads, group_size, head_dim
    )
    key_rows = key_rot.astype(jnp.bfloat16).reshape(rows_dev, block_len, kv_heads * head_dim)
    values = value_raw.astype(jnp.bfloat16).reshape(rows_dev, block_len, kv_heads * head_dim)
    keys_all, values_all = (
        lax.all_gather(key_rows, "ctx", axis=1, tiled=True),
        lax.all_gather(values, "ctx", axis=1, tiled=True),
    )

    def key_tile(tile_index):
        tile_start = tile_index * key_block
        key_pos = tile_start + jnp.arange(key_block, dtype=jnp.int32)
        key_part = lax.dynamic_slice_in_dim(keys_all, tile_start, key_block, 1).reshape(
            rows_dev, key_block, kv_heads, head_dim
        )
        value_part = lax.dynamic_slice_in_dim(values_all, tile_start, key_block, 1).reshape(
            rows_dev, key_block, kv_heads, head_dim
        )
        scores = (
            jnp.einsum("rqhgd,rkhd->rhgqk", queries, key_part, preferred_element_type=jnp.float32)
            * score_scale
        )
        allowed = (key_pos[None, None, :] <= slot_pos[None, :, None]) & (
            key_pos[None, None, :] < lengths[:, None, None]
        )
        return (tile_start, scores, allowed[:, None, None], key_part, value_part)

    stat_shape = (rows_dev, kv_heads, group_size, block_len)

    def stats_step(tile_index, carried):
        running_max, running_sum = carried
        tile_start, scores, allowed, key_part, value_part = key_tile(tile_index)
        masked = jnp.where(allowed, scores, NEGATIVE)
        new_max = jnp.maximum(running_max, jnp.max(masked, axis=-1))
        terms = jnp.where(allowed, jnp.exp(masked - new_max[..., None]), 0.0)
        return (new_max, running_sum * jnp.exp(running_max - new_max) + jnp.sum(terms, axis=-1))

    running_max, running_sum = lax.fori_loop(
        0,
        tiles_used,
        stats_step,
        (jnp.full(stat_shape, NEGATIVE, jnp.float32), jnp.zeros(stat_shape, jnp.float32)),
    )
    log_total = running_max + jnp.log(running_sum)
    out_shape = (rows_dev, block_len, kv_heads, group_size, head_dim)

    def value_step(tile_index, carried):
        rounded_out, exact_out = carried
        tile_start, scores, allowed, key_part, value_part = key_tile(tile_index)
        tile_probs = jnp.where(allowed, jnp.exp(scores - log_total[..., None]), 0.0)
        rounded_out = rounded_out + jnp.einsum(
            "rhgqk,rkhd->rqhgd",
            tile_probs.astype(jnp.bfloat16),
            value_part,
            preferred_element_type=jnp.float32,
        )
        exact_out = exact_out + jnp.einsum(
            "rhgqk,rkhd->rqhgd", tile_probs, value_part.astype(jnp.float32)
        )
        return (rounded_out, exact_out)

    rounded_out, exact_out = lax.fori_loop(
        0,
        tiles_used,
        value_step,
        (jnp.zeros(out_shape, jnp.float32), jnp.zeros(out_shape, jnp.float32)),
    )
    attended = rounded_out.astype(jnp.bfloat16).reshape(count_tok, q_heads * head_dim)
    attn_total = lax.psum(linear(attended, w_output), "tp")
    resid = inputs + attn_total.reshape(rows_dev, block_len, model_width)
    normed_two, back_two = jax.vjp(rms_scale, resid, gain_two_f)
    normed_second = normed_two.astype(jnp.bfloat16).reshape(count_tok, model_width)
    gate_act = linear(normed_second, w_gate)
    up_act = linear(normed_second, w_upper)
    hidden_full, back_glu = jax.vjp(swiglu, gate_act, up_act)
    hidden = hidden_full.astype(jnp.bfloat16)
    ffn_total = lax.psum(linear(hidden, w_down), "tp")
    result = resid + ffn_total.reshape(rows_dev, block_len, model_width)
    error_value = result - teacher.astype(jnp.float32)
    valid_col = valid[..., None]
    total_square, total_count = lax.psum(
        (jnp.sum(valid_col * error_value * error_value), jnp.sum(valid)), ("fsdp", "ctx")
    )
    teacher_loss = total_square / (total_count * model_width)
    grad_result = valid_col * error_value * (slots / total_count)
    grad_low = grad_result.astype(jnp.bfloat16).reshape(count_tok, model_width)
    grad_down = linear_left(hidden, grad_low)
    grad_hidden = linear_right(grad_low, w_down)
    grad_gate_full, grad_up_full = back_glu(grad_hidden)
    grad_gate = grad_gate_full.astype(jnp.bfloat16)
    grad_up = grad_up_full.astype(jnp.bfloat16)
    grad_wgate = linear_left(normed_second, grad_gate)
    grad_wup = linear_left(normed_second, grad_up)
    normed_two_part = linear_right(grad_gate, w_gate) + linear_right(grad_up, w_upper)
    grad_normed_two = lax.psum(normed_two_part, "tp")
    grad_resid_norm, grad_gain_two = back_two(
        grad_normed_two.reshape(rows_dev, block_len, model_width)
    )
    grad_resid = grad_result + grad_resid_norm
    grad_attn_low = grad_resid.astype(jnp.bfloat16).reshape(count_tok, model_width)
    grad_woutput = linear_left(attended, grad_attn_low)
    grad_attended = linear_right(grad_attn_low, w_output).astype(jnp.bfloat16).reshape(out_shape)
    delta = jnp.einsum("rqhgd,rqhgd->rhgq", grad_attended.astype(jnp.float32), exact_out)
    full_shape = (rows_dev, row_len, kv_heads * head_dim)

    def grad_step(tile_index, carried):
        grad_queries, grad_keys, grad_values = carried
        tile_start, scores, allowed, key_part, value_part = key_tile(tile_index)
        tile_probs = jnp.where(allowed, jnp.exp(scores - log_total[..., None]), 0.0)
        grad_probs = jnp.einsum(
            "rqhgd,rkhd->rhgqk", grad_attended, value_part, preferred_element_type=jnp.float32
        )
        grad_scores = (tile_probs * (grad_probs - delta[..., None])).astype(jnp.bfloat16)
        grad_queries = (
            grad_queries
            + jnp.einsum(
                "rhgqk,rkhd->rqhgd", grad_scores, key_part, preferred_element_type=jnp.float32
            )
            * score_scale
        )
        key_term = (
            jnp.einsum(
                "rhgqk,rqhgd->rkhd", grad_scores, queries, preferred_element_type=jnp.float32
            )
            * score_scale
        )
        value_term = jnp.einsum(
            "rhgqk,rqhgd->rkhd",
            tile_probs.astype(jnp.bfloat16),
            grad_attended,
            preferred_element_type=jnp.float32,
        )
        grad_keys = lax.dynamic_update_slice_in_dim(
            grad_keys, key_term.reshape(rows_dev, key_block, kv_heads * head_dim), tile_start, 1
        )
        grad_values = lax.dynamic_update_slice_in_dim(
            grad_values, value_term.reshape(rows_dev, key_block, kv_heads * head_dim), tile_start, 1
        )
        return (grad_queries, grad_keys, grad_values)

    grad_queries, grad_keys, grad_values = lax.fori_loop(
        0,
        tiles_used,
        grad_step,
        (
            jnp.zeros(out_shape, jnp.float32),
            jnp.zeros(full_shape, jnp.float32),
            jnp.zeros(full_shape, jnp.float32),
        ),
    )
    key_grad, value_grad = (
        lax.psum_scatter(grad_keys, "ctx", scatter_dimension=1, tiled=True),
        lax.psum_scatter(grad_values, "ctx", scatter_dimension=1, tiled=True),
    )
    grad_query_raw, grad_gain_query = query_back(
        grad_queries.reshape(rows_dev, block_len, q_heads, head_dim)
    )
    grad_key_raw, grad_gain_key = key_back(
        key_grad.reshape(rows_dev, block_len, kv_heads, head_dim)
    )
    query_low = grad_query_raw.astype(jnp.bfloat16)
    key_low = grad_key_raw.astype(jnp.bfloat16)
    value_low = value_grad.reshape(count_tok, kv_heads * head_dim).astype(jnp.bfloat16)
    grad_wquery = linear_left(normed_low, query_low)
    grad_wkey = linear_left(normed_low, key_low)
    grad_wvalue = linear_left(normed_low, value_low)
    normed_part = (
        linear_right(query_low, w_query)
        + linear_right(key_low, w_key)
        + linear_right(value_low, w_value)
    )
    grad_normed_one, grad_gain_query, grad_gain_key = lax.psum(
        (normed_part, grad_gain_query, grad_gain_key), "tp"
    )
    grad_input_norm, grad_gain_one = back_one(
        grad_normed_one.reshape(rows_dev, block_len, model_width)
    )
    tokens_grad = grad_resid + grad_input_norm
    partials = (
        grad_gain_one,
        grad_wquery,
        grad_wkey,
        grad_wvalue,
        grad_gain_query,
        grad_gain_key,
        grad_woutput,
        grad_gain_two,
        grad_wgate,
        grad_wup,
        grad_down,
    )
    pieces = (
        lax.psum_scatter(partials[0], ("fsdp", "ctx"), scatter_dimension=0, tiled=True),
        lax.psum_scatter(partials[1], ("fsdp", "ctx"), scatter_dimension=0, tiled=True),
        lax.psum_scatter(partials[2], ("fsdp", "ctx"), scatter_dimension=0, tiled=True),
        lax.psum_scatter(partials[3], ("fsdp", "ctx"), scatter_dimension=0, tiled=True),
        lax.psum_scatter(partials[4], ("fsdp", "ctx"), scatter_dimension=0, tiled=True),
        lax.psum_scatter(partials[5], ("fsdp", "ctx"), scatter_dimension=0, tiled=True),
        lax.psum_scatter(partials[6], ("fsdp", "ctx"), scatter_dimension=1, tiled=True),
        lax.psum_scatter(partials[7], ("fsdp", "ctx"), scatter_dimension=0, tiled=True),
        lax.psum_scatter(partials[8], ("fsdp", "ctx"), scatter_dimension=0, tiled=True),
        lax.psum_scatter(partials[9], ("fsdp", "ctx"), scatter_dimension=0, tiled=True),
        lax.psum_scatter(partials[10], ("fsdp", "ctx"), scatter_dimension=1, tiled=True),
    )
    summed = (
        lax.all_gather(pieces[0], "ctx", axis=0, tiled=True),
        lax.all_gather(pieces[1], "ctx", axis=0, tiled=True),
        lax.all_gather(pieces[2], "ctx", axis=0, tiled=True),
        lax.all_gather(pieces[3], "ctx", axis=0, tiled=True),
        lax.all_gather(pieces[4], "ctx", axis=0, tiled=True),
        lax.all_gather(pieces[5], "ctx", axis=0, tiled=True),
        lax.all_gather(pieces[6], "ctx", axis=1, tiled=True),
        lax.all_gather(pieces[7], "ctx", axis=0, tiled=True),
        lax.all_gather(pieces[8], "ctx", axis=0, tiled=True),
        lax.all_gather(pieces[9], "ctx", axis=0, tiled=True),
        lax.all_gather(pieces[10], "ctx", axis=1, tiled=True),
    )
    return (
        result.astype(jnp.bfloat16),
        teacher_loss,
        tokens_grad,
        summed[0],
        summed[1],
        summed[2],
        summed[3],
        summed[4],
        summed[5],
        summed[6],
        summed[7],
        summed[8],
        summed[9],
        summed[10],
    )


BF16 = jnp.bfloat16
F32 = jnp.float32
LOG2E = math.log2(math.e)
X_SWAP = [(0, 2), (2, 0), (1, 3), (3, 1)]
CORE_SWAP = [(0, 1), (1, 0), (2, 3), (3, 2)]
Y_SWAP = [(0, 1), (1, 0)]
Z_UP = [(0, 1), (1, 2), (2, 3), (3, 0)]
Z_DOWN = [(0, 3), (1, 0), (2, 1), (3, 2)]
Z_NEAR = [(0, 1), (1, 0), (2, 3), (3, 2)]
Z_FAR = [(0, 2), (2, 0), (1, 3), (3, 1)]
MASKS = (0, 2, 1, 3)
ANY = pl.BlockSpec(memory_space=pl.ANY)
SMEM = pl.BlockSpec(memory_space=pltpu.SMEM)


def fits(mesh):
    return dict(mesh.shape) == {"fsdp": 4, "ctx": 2, "tp": 4}


def dot(left, right, left_dim, right_dim):
    return lax.dot_general(
        left, right, (((left_dim,), (right_dim,)), ((), ())), preferred_element_type=F32
    )


def sigmoid(v):
    return 0.5 * jnp.tanh(0.5 * v) + 0.5


def whole(shape):
    zeros = (0,) * len(shape)
    return pl.BlockSpec(shape, lambda *_: zeros, pipeline_mode=pl.Buffered(1))


def settings(dims, mib):
    return pltpu.CompilerParams(
        dimension_semantics=("arbitrary",) * dims, vmem_limit_bytes=max(mib, 60) << 20
    )


def shape_of(shape, dtype):
    return jax.ShapeDtypeStruct(shape, dtype)


def cost(flops, bytes_accessed):
    return pl.CostEstimate(
        flops=max(flops, 1 << 42), bytes_accessed=max(bytes_accessed, 1 << 30), transcendentals=0
    )


def pack_kernel(info, o_in, g_in, u_in, d_in, out_ref, ffn_ref, o_ref, g_ref, u_ref, d_ref, sems):
    ctx = info[2]
    pairs = ((o_in, o_ref), (g_in, g_ref), (u_in, u_ref), (d_in, d_ref))
    copies = [pltpu.make_async_copy(a, b, sems.at[i]) for i, (a, b) in enumerate(pairs)]
    for copy in copies:
        copy.start()
    for copy in copies:
        copy.wait()
    out_ref[...] = o_ref[...].astype(F32).T.astype(BF16)
    third = g_ref.shape[1] // 3
    for j in range(3):
        at = pl.multiple_of(jnp.where(ctx == 0, j, 2 - j) * third, third)
        base = 3 * third * j
        ffn_ref[:, base : base + third] = g_ref[:, pl.ds(at, third)]
        ffn_ref[:, base + third : base + 2 * third] = u_ref[:, pl.ds(at, third)]
        down = d_ref[pl.ds(at, third), :].astype(F32).T.astype(BF16)
        ffn_ref[:, base + 2 * third : base + 3 * third] = down


def pack(info, o, g, u, d):
    rows = g.shape[0]
    return pl.pallas_call(
        pack_kernel,
        in_specs=[SMEM] + [ANY] * 4,
        out_specs=[pl.BlockSpec(memory_space=pltpu.VMEM)] * 2,
        out_shape=[shape_of((rows, o.shape[0]), BF16), shape_of((rows, 3 * g.shape[1]), BF16)],
        scratch_shapes=[pltpu.VMEM(a.shape, BF16) for a in (o, g, u, d)]
        + [pltpu.SemaphoreType.DMA((4,))],
        compiler_params=pltpu.CompilerParams(vmem_limit_bytes=60 << 20),
        cost_estimate=cost(0, 6 << 20),
        name="pack",
    )(info, o, g, u, d)


def norm_one_kernel(info, tok_ref, gain_ref, x_ref, nt_ref, x32):
    quarter = x_ref.shape[1] // 4
    for p, mask in enumerate(MASKS):
        at = pl.multiple_of(jnp.bitwise_xor(info[1], mask) * quarter, quarter)
        part = tok_ref[0, :, pl.ds(at, quarter)]
        x_ref[:, p * quarter : (p + 1) * quarter] = part
        x32[:, p * quarter : (p + 1) * quarter] = part.astype(F32)
    x = x32[...]
    rho = lax.rsqrt(jnp.mean(x * x, axis=-1, keepdims=True) + EPS)
    nt_ref[...] = (x * rho * gain_ref[...]).T.astype(BF16)


def norm_one(info, tokens, gain, tile):
    _, tok, width = tokens.shape
    return pl.pallas_call(
        norm_one_kernel,
        grid_spec=pltpu.PrefetchScalarGridSpec(
            num_scalar_prefetch=1,
            grid=(tok // tile,),
            in_specs=[
                pl.BlockSpec((1, tile, width), lambda i, info: (info[0], i, 0)),
                pl.BlockSpec((1, width), lambda i, info: (0, 0)),
            ],
            out_specs=[
                pl.BlockSpec((tile, width), lambda i, info: (i, 0)),
                pl.BlockSpec((width, tile), lambda i, info: (0, i)),
            ],
            scratch_shapes=[pltpu.VMEM((tile, width), F32)],
        ),
        out_shape=[shape_of((tok, width), BF16), shape_of((width, tok), BF16)],
        compiler_params=settings(1, 24),
        cost_estimate=cost(0, 6 << 20),
        name="norm_one",
    )(info, tokens, gain)


def proj_kernel(heads, block, info, *refs):
    pieces = [refs[4 * k : 4 * k + 4] for k in range(4)]
    nt_ref, cos_ref, sin_ref, qg_ref, kg_ref, rot_ref, raw_ref, w_ref, sem = refs[16:]
    rows = w_ref.shape[0] // 4

    @pl.when(pl.program_id(0) == 0)
    def _():
        for k in range(4):

            @pl.when(block(info) == k)
            def _():
                for p, piece in enumerate(pieces[k]):
                    pltpu.make_async_copy(piece, w_ref.at[pl.ds(p * rows, rows)], sem).start()

        pltpu.make_async_copy(w_ref, w_ref, sem).wait()

    hd = qg_ref.shape[0]
    half = hd // 2
    raw = dot(w_ref[...], nt_ref[...], 0, 0)
    cos_part, sin_part = cos_ref[...], sin_ref[...]
    heads_q, heads_k = heads
    raw_ref[...] = raw.astype(BF16)
    for h in range(heads_q + heads_k):
        v = raw[h * hd : (h + 1) * hd]
        rho = lax.rsqrt(jnp.mean(v * v, axis=0, keepdims=True) + EPS)
        v = v * rho * (qg_ref[...] if h < heads_q else kg_ref[...])
        a, b = v[:half], v[half:]
        rot_ref[h * hd : h * hd + half, :] = (a * cos_part - b * sin_part).astype(BF16)
        rot_ref[h * hd + half : (h + 1) * hd, :] = (b * cos_part + a * sin_part).astype(BF16)
    at = (heads_q + heads_k) * hd
    rot_ref[at:, :] = raw[at:].astype(BF16)


def project(info, pieces, normed_t, cos_part, sin_part, gain_q, gain_k, heads, block):
    width, tok = normed_t.shape
    cols = pieces[0][0].shape[1]
    tile = min(512, tok)
    const = lambda a: pl.BlockSpec(a.shape, lambda i, info: (0, 0))
    tab = lambda a: pl.BlockSpec((a.shape[0], tile), lambda i, info: (0, i))
    return pl.pallas_call(
        functools.partial(proj_kernel, heads, block),
        grid_spec=pltpu.PrefetchScalarGridSpec(
            num_scalar_prefetch=1,
            grid=(tok // tile,),
            in_specs=[ANY] * 16
            + [tab(normed_t), tab(cos_part), tab(sin_part), const(gain_q), const(gain_k)],
            out_specs=[pl.BlockSpec((cols, tile), lambda i, info: (0, i))] * 2,
            scratch_shapes=[pltpu.VMEM((width, cols), BF16), pltpu.SemaphoreType.DMA],
        ),
        out_shape=[shape_of((cols, tok), BF16), shape_of((cols, tok), BF16)],
        compiler_params=settings(1, 24),
        cost_estimate=cost(2 * width * cols * tok, 6 << 20),
        name="project",
    )(info, *[p for b in pieces for p in b], normed_t, cos_part, sin_part, gain_q, gain_k)


def head_back_kernel(
    heads, info, dm_ref, dt_ref, rm_ref, rt_ref, cos_ref, sin_ref, qg_ref, kg_ref, out_ref, gg_ref
):
    step, part = pl.program_id(0), pl.program_id(1)
    hd = qg_ref.shape[0]
    half = hd // 2
    heads_q, heads_k = heads
    cos_part, sin_part = cos_ref[...], sin_ref[...]
    tile = cos_part.shape[1]

    @pl.when((step == 0) & (part == 0))
    def _():
        gg_ref[...] = jnp.zeros_like(gg_ref)

    def work(d_ref, r_ref):
        gain_q = jnp.zeros((hd, 1), F32)
        gain_k = jnp.zeros((hd, 1), F32)
        done = []
        for h in range(heads_q + heads_k):
            is_q = h < heads_q
            g = d_ref[h * hd : (h + 1) * hd, :].astype(F32)
            raw = r_ref[h * hd : (h + 1) * hd, :].astype(F32)
            a, b = g[:half], g[half:]
            turned = jnp.concatenate(
                [a * cos_part + b * sin_part, b * cos_part - a * sin_part], axis=0
            )
            rho = lax.rsqrt(jnp.mean(raw * raw, axis=0, keepdims=True) + EPS)
            unit = raw * rho
            prod = turned * unit
            scaled = turned * (qg_ref[...] if is_q else kg_ref[...])
            mean = jnp.mean(scaled * unit, axis=0, keepdims=True)
            done.append(rho * (scaled - unit * mean))
            total = jnp.sum(prod, axis=1, keepdims=True)
            if is_q:
                gain_q = gain_q + total
            else:
                gain_k = gain_k + total
        done.append(d_ref[(heads_q + heads_k) * hd :, :].astype(F32))
        out_ref[0] = jnp.concatenate(done, axis=0).T.astype(BF16)
        lane = lax.broadcasted_iota(jnp.int32, gg_ref.shape, 1)
        gg_ref[...] += jnp.where(lane == 0, gain_q, jnp.where(lane == 1, gain_k, 0.0))

    @pl.when(step == 0)
    def _():
        work(dm_ref, rm_ref)

    @pl.when(step == 1)
    def _():
        work(dt_ref, rt_ref)


def head_back(info, grad_mine, grad_theirs, raw_mine, raw_theirs, cos_part, sin_part, gq, gk, heads):
    cols, tok = grad_mine.shape
    tile = min(512, tok)
    mine = pl.BlockSpec((cols, tile), lambda s, i, info: (0, jnp.where(s == 0, i, tok // tile - 1)))
    theirs = pl.BlockSpec((cols, tile), lambda s, i, info: (0, jnp.where(s == 0, 0, i)))
    tab = lambda a: pl.BlockSpec((a.shape[0], tile), lambda s, i, info: (0, i))
    const = lambda a: pl.BlockSpec(a.shape, lambda s, i, info: (0, 0))
    return pl.pallas_call(
        functools.partial(head_back_kernel, heads),
        grid_spec=pltpu.PrefetchScalarGridSpec(
            num_scalar_prefetch=1,
            grid=(2, tok // tile),
            in_specs=[
                mine,
                theirs,
                mine,
                theirs,
                tab(cos_part),
                tab(sin_part),
                const(gq),
                const(gk),
            ],
            out_specs=[
                pl.BlockSpec(
                    (1, tile, cols), lambda s, i, info: (jnp.bitwise_xor(info[2], s), i, 0)
                ),
                pl.BlockSpec((gq.shape[0], 128), lambda s, i, info: (0, 0)),
            ],
        ),
        out_shape=[shape_of((2, tok, cols), BF16), shape_of((gq.shape[0], 128), F32)],
        compiler_params=settings(2, 24),
        cost_estimate=cost(0, 8 << 20),
        name="head_back",
    )(info, grad_mine, grad_theirs, raw_mine, raw_theirs, cos_part, sin_part, gq, gk)


def load_rows(info, mine_ref, got_ref, rows, sems):
    tok = mine_ref.shape[1]
    ctx = info[2]
    here = pl.multiple_of(ctx * tok, tok)
    there = pl.multiple_of((1 - ctx) * tok, tok)
    one = pltpu.make_async_copy(mine_ref, rows.at[:, pl.ds(here, tok)], sems.at[0])
    two = pltpu.make_async_copy(got_ref, rows.at[:, pl.ds(there, tok)], sems.at[1])
    one.start()
    two.start()
    one.wait()
    two.wait()


def keys_with_bias(keys, length):
    hd, slots = keys.shape
    pos = lax.broadcasted_iota(jnp.int32, (hd, slots), 1)
    row = lax.broadcasted_iota(jnp.int32, (hd, slots), 0)
    bias = jnp.where((row == 0) & (pos >= length), NEGATIVE, 0.0)
    return jnp.concatenate([keys.astype(F32), bias], axis=0).T.astype(BF16)


def query_with_one(pair):
    one_row = jnp.where(lax.broadcasted_iota(jnp.int32, pair.shape, 0) == 0, 1.0, 0.0)
    return jnp.concatenate([pair, one_row.astype(BF16)], axis=0)


def causal(scores, width):
    key_pos = lax.broadcasted_iota(jnp.int32, (width, width), 0)
    query_pos = lax.broadcasted_iota(jnp.int32, (width, width), 1)
    allowed = key_pos <= query_pos
    return jnp.where(jnp.concatenate([allowed, allowed], axis=1), scores, NEGATIVE)


def attn_fwd_kernel(
    width, hd, info, mine_ref, got_ref, keep_ref, send_ref, lse_ref, rows, key_rows, sems
):
    head, block = pl.program_id(0), pl.program_id(1)
    heads_k = pl.num_programs(0)
    scale = hd**-0.5 * LOG2E
    length = info[3]
    key_at = pl.multiple_of(heads_k * 2 * hd + head * hd, hd)
    value_at = pl.multiple_of(heads_k * 3 * hd + head * hd, hd)
    query_at = pl.multiple_of(head * 2 * hd, 2 * hd)

    @pl.when((head == 0) & (block == 0))
    def _():
        load_rows(info, mine_ref, got_ref, rows, sems)

    @pl.when(block == 0)
    def _():
        key_rows[...] = keys_with_bias(rows[pl.ds(key_at, hd), :], length)

    start = pl.multiple_of(block * width, width)
    both = rows[pl.ds(query_at, 2 * hd), pl.ds(start, width)]
    query = query_with_one(jnp.concatenate([both[:hd], both[hd:]], axis=1))

    def tile(at, carried, diagonal):
        out, total = carried
        scores = dot(key_rows[pl.ds(at, width), :], query, 1, 0)
        if diagonal:
            scores = causal(scores, width)
        probs = jnp.exp2(scores * scale)
        total = total + jnp.sum(probs, axis=0, keepdims=True)
        out = out + dot(rows[pl.ds(value_at, hd), pl.ds(at, width)], probs.astype(BF16), 1, 0)
        return out, total

    carried = (jnp.zeros((hd, 2 * width), F32), jnp.zeros((1, 2 * width), F32))
    full = jnp.minimum(block, lax.div(length + width - 1, width))
    carried = lax.fori_loop(
        0, full, lambda j, c: tile(pl.multiple_of(j * width, width), c, False), carried
    )
    out, total = tile(start, carried, True)
    out = out * (1.0 / total)
    out = jnp.concatenate([out[:, :width], out[:, width:]], axis=0).T.astype(BF16)
    here = block // 2 == info[2]

    @pl.when(here)
    def _():
        keep_ref[...] = out

    @pl.when(jnp.logical_not(here))
    def _():
        send_ref[...] = out

    log_total = jnp.log2(total)
    lse_ref[0, 0:1, :] = log_total[:, :width]
    lse_ref[0, 1:2, :] = log_total[:, width:]


def keep_block(i, info):
    return jnp.clip(i - 2 * info[2], 0, 1)


def send_block(i, info):
    return jnp.clip(i - 2 * (1 - info[2]), 0, 1)


def attn_fwd(info, mine, got, hd):
    cols, tok = mine.shape
    heads_k = cols // (4 * hd)
    width = tok // 2
    return pl.pallas_call(
        functools.partial(attn_fwd_kernel, width, hd),
        grid_spec=pltpu.PrefetchScalarGridSpec(
            num_scalar_prefetch=1,
            grid=(heads_k, 4),
            in_specs=[ANY, ANY],
            out_specs=[
                pl.BlockSpec((width, 2 * hd), lambda h, i, info: (keep_block(i, info), h)),
                pl.BlockSpec((width, 2 * hd), lambda h, i, info: (send_block(i, info), h)),
                pl.BlockSpec((1, 2, width), lambda h, i, info: (h, 0, i)),
            ],
            scratch_shapes=[
                pltpu.VMEM((cols, 2 * tok), BF16),
                pltpu.VMEM((2 * tok, 2 * hd), BF16),
                pltpu.SemaphoreType.DMA((2,)),
            ],
        ),
        out_shape=[
            shape_of((tok, heads_k * 2 * hd), BF16),
            shape_of((tok, heads_k * 2 * hd), BF16),
            shape_of((heads_k, 2, 2 * tok), F32),
        ],
        compiler_params=settings(2, 32),
        cost_estimate=cost(heads_k * 2 * tok * 2 * tok * 256 * 4, 8 << 20),
        name="attn_fwd",
    )(info, mine, got)


def attn_bwd_kernel(
    width,
    hd,
    info,
    mine_ref,
    got_ref,
    ok_ref,
    os_ref,
    gk_ref,
    gs_ref,
    lse_ref,
    keep_ref,
    send_ref,
    rows,
    key_rows,
    value_rows,
    key_sum,
    value_sum,
    sems,
):
    head, block = pl.program_id(0), pl.program_id(1)
    heads_k = pl.num_programs(0)
    scale = hd**-0.5
    length = info[3]
    ctx = info[2]
    tok = keep_ref.shape[1]
    key_at = pl.multiple_of(heads_k * 2 * hd + head * hd, hd)
    value_at = pl.multiple_of(heads_k * 3 * hd + head * hd, hd)
    query_at = pl.multiple_of(head * 2 * hd, 2 * hd)

    @pl.when((head == 0) & (block == 0))
    def _():
        load_rows(info, mine_ref, got_ref, rows, sems)

    @pl.when(block == 0)
    def _():
        key_rows[...] = keys_with_bias(rows[pl.ds(key_at, hd), :], length)
        value_rows[...] = rows[pl.ds(value_at, hd), :].astype(F32).T.astype(BF16)
        key_sum[...] = jnp.zeros_like(key_sum)
        value_sum[...] = jnp.zeros_like(value_sum)

    start = pl.multiple_of(block * width, width)
    here = block // 2 == ctx

    def store_query(value):
        at = pl.ds(pl.multiple_of((block % 2) * width, width), width)

        @pl.when(here)
        def _():
            keep_ref[pl.ds(query_at, 2 * hd), at] = value

        @pl.when(jnp.logical_not(here))
        def _():
            send_ref[pl.ds(query_at, 2 * hd), at] = value

    @pl.when(block * width < length)
    def _():
        both = rows[pl.ds(query_at, 2 * hd), pl.ds(start, width)]
        pair = jnp.concatenate([both[:hd], both[hd:]], axis=1)
        query = query_with_one(pair)
        query_rows = pair.astype(F32).T.astype(BF16)
        grad_wide = jnp.where(here, gk_ref[...].astype(F32), gs_ref[...].astype(F32))
        out_wide = jnp.where(here, ok_ref[...].astype(F32), os_ref[...].astype(F32))
        grad_rows = jnp.concatenate([grad_wide[:, :hd], grad_wide[:, hd:]], axis=0).astype(BF16)
        grad_t = grad_wide.T
        prod = (grad_wide * out_wide).T
        grad = jnp.concatenate([grad_t[:hd], grad_t[hd:]], axis=1).astype(BF16)
        delta = jnp.concatenate(
            [
                jnp.sum(prod[:hd], axis=0, keepdims=True),
                jnp.sum(prod[hd:], axis=0, keepdims=True),
            ],
            axis=1,
        )
        lse = jnp.concatenate([lse_ref[0, 0:1, :], lse_ref[0, 1:2, :]], axis=1)

        def tile(at, query_sum, diagonal):
            scores = dot(key_rows[pl.ds(at, width), :], query, 1, 0)
            if diagonal:
                scores = causal(scores, width)
            probs = jnp.exp2(scores * (scale * LOG2E) - lse)
            grad_probs = dot(value_rows[pl.ds(at, width), :], grad, 1, 0)
            grad_scores = (probs * (grad_probs - delta)).astype(BF16)
            value_sum[pl.ds(at, width), :] += dot(probs.astype(BF16), grad_rows, 1, 0)
            key_sum[pl.ds(at, width), :] += dot(grad_scores, query_rows, 1, 0)
            return query_sum + dot(rows[pl.ds(key_at, hd), pl.ds(at, width)], grad_scores, 1, 0)

        query_sum = lax.fori_loop(
            0,
            block,
            lambda j, s: tile(pl.multiple_of(j * width, width), s, False),
            jnp.zeros((hd, 2 * width), F32),
        )
        query_sum = tile(start, query_sum, True) * scale
        store_query(
            jnp.concatenate([query_sum[:, :width], query_sum[:, width:]], axis=0).astype(BF16)
        )

    @pl.when(block * width >= length)
    def _():
        store_query(jnp.zeros((2 * hd, width), BF16))

    @pl.when(block == 3)
    def _():
        for at, total in ((key_at, key_sum[...] * scale), (value_at, value_sum[...])):
            total = total.T.astype(BF16)
            left, right = total[:, :tok], total[:, tok:]

            @pl.when(ctx == 0)
            def _():
                keep_ref[pl.ds(at, hd), :] = left
                send_ref[pl.ds(at, hd), :] = right

            @pl.when(ctx == 1)
            def _():
                keep_ref[pl.ds(at, hd), :] = right
                send_ref[pl.ds(at, hd), :] = left


def attn_bwd(info, mine, got, out_keep, out_send, grad_keep, grad_send, lse, hd):
    cols, tok = mine.shape
    heads_k = cols // (4 * hd)
    width = tok // 2
    keep = pl.BlockSpec((width, 2 * hd), lambda h, i, info: (keep_block(i, info), h))
    send = pl.BlockSpec((width, 2 * hd), lambda h, i, info: (send_block(i, info), h))
    full = pl.BlockSpec((cols, tok), lambda h, i, info: (0, 0))
    return pl.pallas_call(
        functools.partial(attn_bwd_kernel, width, hd),
        grid_spec=pltpu.PrefetchScalarGridSpec(
            num_scalar_prefetch=1,
            grid=(heads_k, 4),
            in_specs=[
                ANY,
                ANY,
                keep,
                send,
                keep,
                send,
                pl.BlockSpec((1, 2, width), lambda h, i, info: (h, 0, i)),
            ],
            out_specs=[full, full],
            scratch_shapes=[
                pltpu.VMEM((cols, 2 * tok), BF16),
                pltpu.VMEM((2 * tok, 2 * hd), BF16),
                pltpu.VMEM((2 * tok, hd), BF16),
                pltpu.VMEM((2 * tok, hd), F32),
                pltpu.VMEM((2 * tok, hd), F32),
                pltpu.SemaphoreType.DMA((2,)),
            ],
        ),
        out_shape=[shape_of((cols, tok), BF16), shape_of((cols, tok), BF16)],
        compiler_params=settings(2, 40),
        cost_estimate=cost(heads_k * 5 * tok * 2 * tok * 256 * 4, 12 << 20),
        name="attn_bwd",
    )(info, mine, got, out_keep, out_send, grad_keep, grad_send, lse)


def load_blocks(pieces, target, sem):
    rows = target.shape[1] // 4

    @pl.when(pl.program_id(0) == 0)
    def _():
        for i, piece in enumerate(pieces):
            block = target.at[i // 4, pl.ds(i % 4 * rows, rows)]
            pltpu.make_async_copy(piece, block, sem).start()
        pltpu.make_async_copy(target, target, sem).wait()


def out_proj_kernel(info, *refs):
    x_ref, a0, a1, b0, b1, gain_ref, r_ref, n_ref, nt_ref, att_ref, w_ref, sem = refs[16:]
    load_blocks(refs[:16], w_ref, sem)
    ctx = info[2]
    total = x_ref[...].astype(F32)
    for j, ref, side in ((0, a0, ctx), (1, a1, ctx), (0, b0, 1 - ctx), (1, b1, 1 - ctx)):
        block = 2 * side + j
        part = ref[...]
        att_ref[block] = part
        total = total + dot(part, w_ref[block], 1, 1)
    rho = lax.rsqrt(jnp.mean(total * total, axis=-1, keepdims=True) + EPS)
    normed = total * rho * gain_ref[...]
    r_ref[...] = total
    n_ref[...] = normed.astype(BF16)
    nt_ref[...] = normed.T.astype(BF16)


def out_proj(info, x, mine, theirs, pieces, gain, tile):
    tok, width = x.shape
    feats = pieces[0][0].shape[1]
    rows_of = lambda n: pl.BlockSpec((tile, n), lambda i, info: (i, 0))
    return pl.pallas_call(
        out_proj_kernel,
        grid_spec=pltpu.PrefetchScalarGridSpec(
            num_scalar_prefetch=1,
            grid=(tok // tile,),
            in_specs=[ANY] * 16
            + [rows_of(width)]
            + [rows_of(feats)] * 4
            + [pl.BlockSpec((1, width), lambda i, info: (0, 0))],
            out_specs=[
                rows_of(width),
                rows_of(width),
                pl.BlockSpec((width, tile), lambda i, info: (0, i)),
                pl.BlockSpec((4, tile, feats), lambda i, info: (0, i, 0)),
            ],
            scratch_shapes=[pltpu.VMEM((4, width, feats), BF16), pltpu.SemaphoreType.DMA],
        ),
        out_shape=[
            shape_of((tok, width), F32),
            shape_of((tok, width), BF16),
            shape_of((width, tok), BF16),
            shape_of((4, tok, feats), BF16),
        ],
        compiler_params=settings(1, 32),
        cost_estimate=cost(2 * tok * width * 4 * feats, 16 << 20),
        name="out_proj",
    )(info, *[p for b in pieces for p in b], x, *mine, *theirs, gain)


def norm_two_back_kernel(info, *refs):
    g_ref, r_ref, gr_ref, gain_ref, gres_ref, gat_ref, a0, a1, b0, b1, gg_ref, w_ref, sem = refs[16:]
    load_blocks(refs[:16], w_ref, sem)
    ctx = info[2]
    grad, resid = g_ref[...], r_ref[...]
    rho = lax.rsqrt(jnp.mean(resid * resid, axis=-1, keepdims=True) + EPS)
    unit = resid * rho
    scaled = grad * gain_ref[...]
    back = rho * (scaled - unit * jnp.mean(scaled * unit, axis=-1, keepdims=True))
    total = gr_ref[...] + back
    gres_ref[...] = total
    low = total.astype(BF16)
    gat_ref[...] = total.T.astype(BF16)

    @pl.when(pl.program_id(0) == 0)
    def _():
        gg_ref[...] = jnp.zeros_like(gg_ref)

    gg_ref[...] += jnp.sum(grad * unit, axis=0, keepdims=True)
    for j, ref, side in ((0, a0, ctx), (1, a1, ctx), (0, b0, 1 - ctx), (1, b1, 1 - ctx)):
        ref[...] = dot(low, w_ref[2 * side + j], 1, 0).astype(BF16)


def norm_two_back(info, grad, resid, grad_result, gain, pieces, tile):
    tok, width = grad.shape
    feats = pieces[0][0].shape[1]
    rows_of = lambda n: pl.BlockSpec((tile, n), lambda i, info: (i, 0))
    row = pl.BlockSpec((1, width), lambda i, info: (0, 0))
    return pl.pallas_call(
        norm_two_back_kernel,
        grid_spec=pltpu.PrefetchScalarGridSpec(
            num_scalar_prefetch=1,
            grid=(tok // tile,),
            in_specs=[ANY] * 16 + [rows_of(width)] * 3 + [row],
            out_specs=[rows_of(width), pl.BlockSpec((width, tile), lambda i, info: (0, i))]
            + [rows_of(feats)] * 4
            + [row],
            scratch_shapes=[pltpu.VMEM((4, width, feats), BF16), pltpu.SemaphoreType.DMA],
        ),
        out_shape=[shape_of((tok, width), F32), shape_of((width, tok), BF16)]
        + [shape_of((tok, feats), BF16)] * 4
        + [shape_of((1, width), F32)],
        compiler_params=settings(1, 32),
        cost_estimate=cost(2 * tok * width * 4 * feats, 24 << 20),
        name="norm_two_back",
    )(info, *[p for b in pieces for p in b], grad, resid, grad_result, gain)


def norm_one_back_kernel(info, *refs):
    p0, p1, x_ref, gres_ref, gain_ref, out_ref, gg_ref, w_ref, sem = refs[16:]
    load_blocks(refs[:16], w_ref, sem)
    quarter = x_ref.shape[1] // 4
    grad = dot(p0[0], w_ref[0], 1, 1)
    grad = grad + dot(p1[0], w_ref[1], 1, 1)
    grad = grad + dot(p0[1], w_ref[2], 1, 1)
    grad = grad + dot(p1[1], w_ref[3], 1, 1)
    x = x_ref[...].astype(F32)
    rho = lax.rsqrt(jnp.mean(x * x, axis=-1, keepdims=True) + EPS)
    unit = x * rho
    scaled = grad * gain_ref[...]
    back = rho * (scaled - unit * jnp.mean(scaled * unit, axis=-1, keepdims=True))
    total = (gres_ref[...] + back).astype(BF16)
    for p, mask in enumerate(MASKS):
        at = pl.multiple_of(jnp.bitwise_xor(info[1], mask) * quarter, quarter)
        out_ref[:, pl.ds(at, quarter)] = total[:, p * quarter : (p + 1) * quarter]

    @pl.when(pl.program_id(0) == 0)
    def _():
        gg_ref[...] = jnp.zeros_like(gg_ref)

    gg_ref[...] += jnp.sum(grad * unit, axis=0, keepdims=True)


def norm_one_back(info, pairs, pieces, x, grad_resid, gain, tile):
    tok, width = x.shape
    cols = pieces[0][0].shape[1]
    rows_of = lambda n: pl.BlockSpec((tile, n), lambda i, info: (i, 0))
    pair = pl.BlockSpec((2, tile, cols), lambda i, info: (0, i, 0))
    row = pl.BlockSpec((1, width), lambda i, info: (0, 0))
    return pl.pallas_call(
        norm_one_back_kernel,
        grid_spec=pltpu.PrefetchScalarGridSpec(
            num_scalar_prefetch=1,
            grid=(tok // tile,),
            in_specs=[ANY] * 16 + [pair, pair, rows_of(width), rows_of(width), row],
            out_specs=[rows_of(width), row],
            scratch_shapes=[pltpu.VMEM((4, width, cols), BF16), pltpu.SemaphoreType.DMA],
        ),
        out_shape=[shape_of((tok, width), BF16), shape_of((1, width), F32)],
        compiler_params=settings(1, 32),
        cost_estimate=cost(2 * tok * width * 4 * cols, 18 << 20),
        name="norm_one_back",
    )(info, *[p for b in pieces for p in b], *pairs, x, grad_resid, gain)


def weight_copies(plan, pieces, gate_up, down, gate_up_sem, down_sem):
    third = down.shape[1] // 3
    rows = down.shape[0] // 4
    wide, thin = [], []
    for p, chunks in enumerate(plan):
        block = pl.ds(p * rows, rows)
        for j, (piece, at) in enumerate(chunks):
            src = pieces[piece]
            wide.append(
                pltpu.make_async_copy(
                    src.at[:, pl.ds(at, 2 * third)],
                    gate_up.at[block, pl.ds(j * 2 * third, 2 * third)],
                    gate_up_sem,
                )
            )
            thin.append(
                pltpu.make_async_copy(
                    src.at[:, pl.ds(at + 2 * third, third)],
                    down.at[block, pl.ds(j * third, third)],
                    down_sem,
                )
            )
    return wide, thin


def split_act(act):
    third = act.shape[1] // 6
    part = lambda j: act[:, j * third : (j + 1) * third]
    return [(part(0), part(1)), (part(2), part(3)), (part(4), part(5))]


def ffn_fwd_kernel(tile, plans, last, info, scale, x_ref, in_ref, *rest):
    if last:
        teach_ref, rest = rest[0], rest[1:]
    pieces = []
    for plan in plans:
        count = 1 + max(piece for chunks in plan for piece, _ in chunks)
        pieces.append(rest[:count])
        rest = rest[count:]
    act_ref, hid_ref = rest[:2]
    if last:
        out_ref, gres_ref, low_ref, lowt_ref, sq_ref = rest[2:7]
        gate_up, down, total, sems = rest[7:]
    else:
        sum_ref, gate_up, down, total, sems = rest[2:]
    step, part = pl.program_id(0), pl.program_id(1)
    final = len(plans) - 1
    width = x_ref.shape[1]
    quarter = width // 4
    third = down.shape[2] // 3

    def copies(s):
        return weight_copies(
            plans[s], pieces[s], gate_up.at[s], down.at[s], sems.at[s, 0], sems.at[s, 1]
        )

    @pl.when((step == 0) & (part == 0))
    def _():
        for s in range(len(plans)):
            wide, thin = copies(s)
            for copy in wide + thin:
                copy.start()

    for s in range(len(plans)):

        @pl.when((step == s) & (part == 0))
        def _():
            pltpu.make_async_copy(gate_up.at[s], gate_up.at[s], sems.at[s, 0]).wait()
            pltpu.make_async_copy(down.at[s], down.at[s], sems.at[s, 1]).wait()

    rows = pl.ds(pl.multiple_of(part * tile, tile), tile)
    act = dot(x_ref[rows, :], gate_up[step], 1, 0)
    for j, (gate, upper) in enumerate(split_act(act)):
        hid_ref[0, :, j * third : (j + 1) * third] = (gate * sigmoid(gate) * upper).astype(BF16)
    act_ref[0] = act.astype(BF16)
    grown = dot(hid_ref[0], down[step], 1, 1)

    @pl.when(step == 0)
    def _():
        total[rows, :] = in_ref[...] + grown

    @pl.when(step > 0)
    def _():
        total[rows, :] += grown

    @pl.when(step == final)
    def _():
        result = total[rows, :]
        if not last:
            sum_ref[...] = result
            return
        tok = x_ref.shape[0]
        slot = info[2] * tok + part * tile + lax.broadcasted_iota(jnp.int32, (tile, 1), 0)
        valid = jnp.where(slot < info[3], 1.0, 0.0)
        square = jnp.zeros((tile, quarter), F32)
        for p, mask in enumerate(MASKS):
            at = pl.multiple_of(jnp.bitwise_xor(info[1], mask) * quarter, quarter)
            cols = slice(p * quarter, (p + 1) * quarter)
            value = result[:, cols]
            out_ref[:, pl.ds(at, quarter)] = value.astype(BF16)
            error = valid * (value - teach_ref[0, :, pl.ds(at, quarter)].astype(F32))
            square = square + error * error
            grad = error * scale[0]
            gres_ref[:, cols] = grad
            low_ref[:, cols] = grad.astype(BF16)
            lowt_ref[cols, :] = grad.T.astype(BF16)

        @pl.when(part == 0)
        def _():
            sq_ref[...] = jnp.zeros_like(sq_ref)

        sq_ref[...] += jnp.sum(square, axis=0, keepdims=True)


def ffn_fwd(info, scale, x, total, teacher, weights, units, tile):
    tok, width = x.shape
    pieces = [piece for _, group in weights for piece in group]
    count = len(weights)
    last = teacher is not None
    entry = lambda s, i: jnp.where(s == 0, i, tok // tile - 1)
    leave = lambda s, i: jnp.where(s == count - 1, i, 0)
    tiles = lambda n: pl.BlockSpec((tile, n), lambda s, i, info: (leave(s, i), 0))
    slab = lambda n: pl.BlockSpec((1, tile, n), lambda s, i, info: (s, i, 0))
    in_specs = [
        SMEM,
        whole((tok, width)),
        pl.BlockSpec((tile, width), lambda s, i, info: (entry(s, i), 0)),
    ]
    out_specs = [slab(2 * units), slab(units)]
    out_shape = [shape_of((count, tok, 2 * units), BF16), shape_of((count, tok, units), BF16)]
    if last:
        in_specs.append(
            pl.BlockSpec((1, tile, width), lambda s, i, info: (info[0], leave(s, i), 0))
        )
        out_specs += [
            tiles(width),
            tiles(width),
            tiles(width),
            pl.BlockSpec((width, tile), lambda s, i, info: (0, leave(s, i))),
            pl.BlockSpec((1, width // 4), lambda s, i, info: (0, 0)),
        ]
        out_shape += [
            shape_of((tok, width), BF16),
            shape_of((tok, width), F32),
            shape_of((tok, width), BF16),
            shape_of((width, tok), BF16),
            shape_of((1, width // 4), F32),
        ]
    else:
        out_specs.append(tiles(width))
        out_shape.append(shape_of((tok, width), F32))
    return pl.pallas_call(
        functools.partial(ffn_fwd_kernel, tile, [plan for plan, _ in weights], last),
        grid_spec=pltpu.PrefetchScalarGridSpec(
            num_scalar_prefetch=1,
            grid=(count, tok // tile),
            in_specs=in_specs + [ANY] * len(pieces),
            out_specs=out_specs,
            scratch_shapes=[
                pltpu.VMEM((count, width, 2 * units), BF16),
                pltpu.VMEM((count, width, units), BF16),
                pltpu.VMEM((tok, width), F32),
                pltpu.SemaphoreType.DMA((count, 2)),
            ],
        ),
        out_shape=out_shape,
        compiler_params=settings(2, 50),
        cost_estimate=cost(2 * tok * width * units * 3 * count, 20 << 20),
        name="ffn_fwd",
    )(info, scale, x, total, *([teacher] if last else []), *pieces)


def ffn_bwd_kernel(steps, plan, first, low_ref, act_ref, hid_ref, xt_ref, lowt_ref, *rest):
    count = 1 + max(piece for chunks in plan for piece, _ in chunks)
    pieces, rest = rest[:count], rest[count:]
    if not first:
        in_ref, rest = rest[0], rest[1:]
    out_ref, keep_ref, send_ref, gate_up, down, dact_all, hid_all, sems = rest
    step = pl.program_id(0)
    units = down.shape[1]
    third = units // 3
    tile = low_ref.shape[0]

    @pl.when(step == 0)
    def _():
        wide, thin = weight_copies(plan, pieces, gate_up, down, sems.at[0], sems.at[1])
        for copy in thin + wide:
            copy.start()
        pltpu.make_async_copy(down, down, sems.at[1]).wait()

    @pl.when(step < steps)
    def _():
        rows = pl.ds(pl.multiple_of(step * tile, tile), tile)
        grad_hidden = dot(low_ref[...], down[...], 1, 0)
        for j, (gate, upper) in enumerate(split_act(act_ref[0])):
            grad = grad_hidden[:, j * third : (j + 1) * third]
            gate, upper = gate.astype(F32), upper.astype(F32)
            sig = sigmoid(gate)
            silu = gate * sig
            at = 2 * j * third
            dact_all[rows, at : at + third] = (
                grad * upper * (sig + silu - silu * sig)
            ).astype(BF16)
            dact_all[rows, at + third : at + 2 * third] = (grad * silu).astype(BF16)
        hid_all[rows, :] = hid_ref[0]

        @pl.when(step == 0)
        def _():
            pltpu.make_async_copy(gate_up, gate_up, sems.at[0]).wait()

        grown = dot(dact_all[rows, :], gate_up[...], 1, 1)
        out_ref[...] = grown if first else in_ref[...] + grown

    def weight_rows(target):
        target[:, : 2 * units] = dot(xt_ref[...], dact_all[...], 1, 0).astype(BF16)
        target[:, 2 * units :] = dot(lowt_ref[...], hid_all[...], 1, 0).astype(BF16)

    @pl.when((step >= steps) & (step < steps + 2))
    def _():
        weight_rows(send_ref)

    @pl.when(step >= steps + 2)
    def _():
        weight_rows(keep_ref)


def ffn_bwd(low, saved, weights, total, xt, lowt, tile):
    plan, pieces = weights
    acts, hiddens, block = saved
    tok, width = low.shape
    units = hiddens.shape[2]
    steps = tok // tile
    quarter = width // 4
    first = total is None
    clip = lambda i: jnp.minimum(i, steps - 1)
    rows_of = lambda n: pl.BlockSpec((tile, n), lambda i: (clip(i), 0))
    slab = lambda n: pl.BlockSpec((1, tile, n), lambda i: (block, clip(i), 0))
    feature = lambda i: (jnp.where(i < steps + 2, jnp.maximum(i - steps, 0) + 2, i - steps - 2), 0)
    return pl.pallas_call(
        functools.partial(ffn_bwd_kernel, steps, plan, first),
        grid=(steps + 4,),
        in_specs=[
            rows_of(width),
            slab(2 * units),
            slab(units),
            pl.BlockSpec((quarter, tok), feature),
            pl.BlockSpec((quarter, tok), feature),
        ]
        + [ANY] * len(pieces)
        + ([] if first else [rows_of(width)]),
        out_specs=[
            rows_of(width),
            pl.BlockSpec((quarter, 3 * units), lambda i: (jnp.maximum(i - steps - 2, 0), 0)),
            pl.BlockSpec((quarter, 3 * units), lambda i: (jnp.clip(i - steps, 0, 1), 0)),
        ],
        out_shape=[
            shape_of((tok, width), F32),
            shape_of((width // 2, 3 * units), BF16),
            shape_of((width // 2, 3 * units), BF16),
        ],
        scratch_shapes=[
            pltpu.VMEM((width, 2 * units), BF16),
            pltpu.VMEM((width, units), BF16),
            pltpu.VMEM((tok, 2 * units), BF16),
            pltpu.VMEM((tok, units), BF16),
            pltpu.SemaphoreType.DMA((2,)),
        ],
        input_output_aliases={} if first else {5 + len(pieces): 0},
        compiler_params=settings(1, 56),
        cost_estimate=cost(2 * tok * width * units * 6, 32 << 20),
        name="ffn_bwd",
    )(low, acts, hiddens, xt, lowt, *pieces, *([] if first else [total]))


def turn_chunks(block):
    wide = block.shape[1] * 2 // 9
    thin = wide // 2
    starts = [(2 * wide, wide), (wide, wide), (0, wide)]
    starts += [(3 * wide + 2 * thin, thin), (3 * wide + thin, thin), (3 * wide, thin)]
    return jnp.concatenate([block[:, a : a + n] for a, n in starts], axis=1)


def sum_kernel(side, turn, info, left_ref, right_ref, *outs):
    right = right_ref[...]
    if turn:
        right = turn_chunks(right)
    total = (left_ref[...].astype(F32) + right.astype(F32)).astype(BF16)
    if len(outs) == 1:
        outs[0][...] = total
        return
    first = side(pl.program_id(0), info) == 0

    @pl.when(first)
    def _():
        outs[0][...] = total

    @pl.when(jnp.logical_not(first))
    def _():
        outs[1][...] = total


def summed(info, left, right, how, turn=False):
    rows, cols = left.shape
    count = rows // 128
    block = lambda at: pl.BlockSpec((128, cols), at)
    if how == "all":
        side, places = None, [lambda i, info: (i, 0)]
    elif how == "halves":
        half = count // 2
        side = lambda i, info: i // half
        places = [
            lambda i, info: (jnp.minimum(i, half - 1), 0),
            lambda i, info: (jnp.maximum(i - half, 0), 0),
        ]
    else:
        side = lambda i, info: jnp.bitwise_xor(i % 2, info[2])
        places = [lambda i, info: (i // 2, 0)] * 2
    shapes = [shape_of((rows // len(places), cols), BF16)] * len(places)
    out = pl.pallas_call(
        functools.partial(sum_kernel, side, turn),
        grid_spec=pltpu.PrefetchScalarGridSpec(
            num_scalar_prefetch=1,
            grid=(count,),
            in_specs=[block(lambda i, info: (i, 0))] * 2,
            out_specs=[block(at) for at in places],
        ),
        out_shape=shapes,
        compiler_params=settings(1, 24),
        cost_estimate=cost(0, 4 << 20),
        name="summed",
    )(info, left, right)
    return out[0] if len(places) == 1 else out


def after(value, *others):
    return lax.optimization_barrier((value,) + others)[0]


def z_gather(block):
    one = lax.ppermute(block, "tp", Z_UP)
    three = lax.ppermute(block, "tp", Z_DOWN)
    two = lax.ppermute(one, "tp", Z_UP)
    return [block, one, two, three]


def add(left, right):
    return left.astype(F32) + right.astype(F32)


def add_low(left, right):
    return add(left, right).astype(BF16)


def z_reduce(parts):
    two = add_low(parts[1], lax.ppermute(parts[2], "tp", Z_DOWN))
    total = add(parts[0], lax.ppermute(two, "tp", Z_DOWN))
    return total + lax.ppermute(parts[3], "tp", Z_UP).astype(F32)


def per_device_rows(
    tokens,
    teacher,
    lengths,
    attn_gain,
    q_weight,
    k_weight,
    v_weight,
    q_gain,
    k_gain,
    o_weight,
    ffn_gain,
    gate_weight,
    up_weight,
    down_weight,
):
    z = lax.axis_index("tp")
    ctx = lax.axis_index("ctx")
    fsdp = lax.axis_index("fsdp")
    rows_dev, tok, width = tokens.shape
    quarter = width // 4
    hd = q_gain.shape[0] * 4
    q_cols, k_cols = q_weight.shape[1], k_weight.shape[1]
    proj = q_cols + 2 * k_cols
    heads = (q_cols // hd, k_cols // hd)
    units = gate_weight.shape[1]
    slots = rows_dev * 4 * tok * 2

    def x_swap(v):
        return lax.ppermute(v, "fsdp", X_SWAP)

    def core_swap(v):
        return lax.ppermute(v, "fsdp", CORE_SWAP)

    def y_swap(v):
        return lax.ppermute(v, "ctx", Y_SWAP)

    length = lax.dynamic_slice_in_dim(lengths, z, 1, 0)
    info = jnp.concatenate([jnp.stack([z, fsdp, ctx]).astype(jnp.int32), length])

    w_proj = jnp.concatenate([q_weight, k_weight, v_weight], axis=1)
    w_out, w_ffn = pack(info, o_weight, gate_weight, up_weight, down_weight)
    count_here = jnp.sum(lengths).astype(F32)[None]
    vector = jnp.concatenate([attn_gain, ffn_gain, q_gain, k_gain]).astype(F32)
    vector = jnp.concatenate([vector, count_here, jnp.zeros((640 - 545,), F32)])[None]
    vector = jnp.concatenate([vector, x_swap(vector)], axis=0)
    vector = jnp.concatenate([vector, core_swap(vector)], axis=0)
    gain_one = vector[:, :quarter].reshape(1, width)
    gain_two = vector[:, quarter : 2 * quarter].reshape(1, width)
    total_count = jnp.sum(vector[:, 544])

    def natural(v):
        v = jnp.concatenate([v[0:1], v[2:3], v[1:2], v[3:4]], axis=0)
        v = jnp.where(fsdp % 2 == 0, v, jnp.concatenate([v[1:2], v[0:1], v[3:4], v[2:3]], axis=0))
        return jnp.where(fsdp // 2 == 0, v, jnp.concatenate([v[2:4], v[0:2]], axis=0))

    head_gains = natural(vector[:, 2 * quarter : 544])
    gain_q = head_gains[:, : hd // 4].reshape(hd, 1)
    gain_k = head_gains[:, hd // 4 :].reshape(hd, 1)

    def z_direct(block):
        return [
            block,
            lax.ppermute(block, "tp", Z_UP),
            lax.ppermute(block, "tp", Z_FAR),
            lax.ppermute(block, "tp", Z_DOWN),
        ]

    def plane_pieces(blocks):
        pieces = []
        for block in blocks:
            far = x_swap(block)
            pieces.append([block, far, core_swap(block), core_swap(far)])
        return pieces

    proj_blocks = z_direct(w_proj)
    proj_pieces = plane_pieces(proj_blocks)
    out_blocks = z_direct(after(w_out, *proj_blocks[1:]))
    ffn_one = lax.ppermute(after(w_ffn, *proj_blocks[1:]), "tp", Z_UP)
    in_block = lambda i: [(i, 0), (i, units), (i, 2 * units)]
    in_pair = lambda i: [(i, 0), (i, units), (i + 1, 0)]
    plan_whole = [in_block(0), in_pair(1), in_block(3), in_pair(4)]
    plan_chunks = [[(3 * p + j, 0) for j in range(3)] for p in range(4)]

    def ffn_pieces(block, far, last):
        return plan_whole, [block, far, last, core_swap(block), core_swap(far), core_swap(last)]

    x_in, normed_one_t = norm_one(info, tokens, gain_one, 256)
    pos = (ctx * tok + jnp.arange(tok, dtype=jnp.int32)).astype(F32)
    frequency = THETA ** (-(2.0 * jnp.arange(hd // 2, dtype=F32)) / hd)
    angles = frequency[:, None] * pos[None, :]
    tables = (jnp.cos(angles), jnp.sin(angles), gain_q, gain_k)

    def make(block, *then):
        return project(info, proj_pieces, after(normed_one_t, *then), *tables, heads, block)

    far_of = lambda block: x_swap(block[:, : 2 * units])
    near = lambda far: far[:, :units]
    own_ffn = after(w_ffn, *[b[1] for b in proj_pieces])
    far0 = far_of(own_ffn)
    weights0 = ffn_pieces(own_ffn, far0, y_swap(near(far0)))

    theirs = [make(lambda s: 2 * (1 - s[2]))]
    theirs.append(make(lambda s: 2 * (1 - s[2]) + 1, theirs[0][0]))
    got = [y_swap(theirs[0][0]), y_swap(theirs[1][0])]
    mine = [make(lambda s: 2 * s[2], theirs[1][0])]
    mine.append(make(lambda s: 2 * s[2] + 1, mine[0][0]))
    out_far = [x_swap(after(block, mine[1][0])) for block in out_blocks]

    ffn_one = after(ffn_one, mine[1][0])
    far1 = far_of(ffn_one)
    ffn_three = lax.ppermute(after(w_ffn, ffn_one, mine[1][0]), "tp", Z_DOWN)
    first = attn_fwd(info, after(mine[0][0], mine[1][0], far0), got[0], hd)
    second = attn_fwd(info, after(mine[1][0], first[1]), got[1], hd)
    out_pieces = []
    for block, far in zip(out_blocks, out_far):
        block, far = after(block, second[1]), after(far, second[1])
        out_pieces.append([block, far, core_swap(block), core_swap(far)])
    outs = [first, second]
    arrived = [y_swap(first[1]), y_swap(second[1])]
    ffn_three = after(ffn_three, second[1])
    far3 = far_of(ffn_three)
    ffn_one, far1 = after(ffn_one, second[1]), after(far1, second[1])
    ffn_two = [
        lax.ppermute(after(ffn_one[:, j * units : (j + 1) * units], ffn_three), "tp", Z_UP)
        for j in range(3)
    ]
    last1 = y_swap(after(near(far1), arrived[1]))
    resid, normed_two, normed_two_t, attended = out_proj(
        info, x_in, [first[0], second[0]], arrived, out_pieces, gain_two, 256
    )

    scale = (slots / total_count)[None]
    weights1 = ffn_pieces(ffn_one, far1, after(last1, normed_two))
    two_first, two_middle = after(ffn_two[0], normed_two), after(ffn_two[1], normed_two)
    two_far = [x_swap(two_first), x_swap(two_middle)]
    far3 = after(far3, normed_two)
    last3 = y_swap(near(far3))
    acts_a, hiddens_a, sum_a = ffn_fwd(
        info, scale, normed_two, resid, None, [weights0, weights1], units, 256
    )
    weights3 = ffn_pieces(ffn_three, far3, after(last3, sum_a))
    two_far = [after(two_far[0], sum_a), after(two_far[1], sum_a)]
    two_far.append(y_swap(two_far[0]))
    acts_b, hiddens_b, sum_b = ffn_fwd(
        info, scale, normed_two, sum_a, None, [weights3], units, 256
    )
    two = [two_first, two_middle, after(ffn_two[2], sum_a)] + two_far[:2] + [after(two_far[2], sum_b)]
    weights2 = (plan_chunks, two + [core_swap(p) for p in two])
    acts_c, hiddens_c, result_low, grad_result, grad_low, grad_low_t, square = ffn_fwd(
        info, scale, normed_two, sum_b, teacher, [weights2], units, 256
    )

    def spread(parts, dtype):
        out = jnp.zeros((rows_dev, tok, width), dtype)
        for k in (0, 1, 3, 2):
            part = parts[k].astype(dtype)[None]
            out = lax.dynamic_update_slice(out, part, (lax.rem(z - k + 4, 4), 0, 0))
        return out

    def ffn_back(weights, saved, total):
        return ffn_bwd(
            grad_low, saved, weights, total, normed_two_t, grad_low_t, 256
        )

    output_one = lax.ppermute(result_low, "tp", Z_UP)
    total, keep2, send2 = ffn_back(weights2, (acts_c, hiddens_c, 0), None)
    came2 = core_swap(send2)
    total, keep1, send1 = ffn_back(weights1, (acts_a, hiddens_a, 1), after(total, send2))
    came1 = core_swap(send1)
    own2, far2 = summed(info, after(keep2, send1), came2, "halves")
    came2 = x_swap(far2)
    output_one = after(output_one, own2)
    output_three = lax.ppermute(after(result_low, output_one), "tp", Z_DOWN)
    total, keep3, send3 = ffn_back(weights3, (acts_b, hiddens_b, 0), after(total, own2, output_one))
    came3 = core_swap(send3)
    here1, there1 = summed(info, after(keep1, send3), came1, "ctx")
    came1 = y_swap(there1)
    total, keep0, send0 = ffn_back(weights0, (acts_a, hiddens_a, 0), after(total, here1))
    came0 = core_swap(send0)
    own3, far3 = summed(info, after(keep3, send0), came3, "halves")
    came3 = x_swap(far3)
    here2, there2 = summed(info, after(own2, own3), came2, "ctx")
    output_three = after(output_three, here2)
    output_two = lax.ppermute(after(output_one, output_three), "tp", Z_UP)
    grad_resid, grad_attn_t, a0, a1, b0, b1, gain_two_sum = norm_two_back(
        info, after(total, here2, output_three), resid, grad_result, gain_two, out_pieces, 256
    )

    grad_got = [y_swap(b0), y_swap(b1)]
    own0, far0 = summed(info, after(keep0, b0), came0, "halves")
    own1, far1 = summed(info, after(here1, own0), came1, "halves", True)
    came1 = x_swap(far1)
    came2 = y_swap(after(there2, grad_got[0]))

    def attn_back(j, grad):
        return attn_bwd(
            info, mine[j][0], got[j], outs[j][0], outs[j][1], grad, grad_got[j], outs[j][2], hd
        )

    first_back = attn_back(0, after(a0, own1))
    grad_heads = [y_swap(first_back[1])]
    part2 = summed(info, after(here2, first_back[1]), came2, "all", True)
    part1 = summed(info, after(own1, part2), came1, "all")
    here3, there3 = summed(info, after(own3, part1), came3, "ctx")
    came0 = x_swap(after(far0, here3))
    output_two = after(output_two, here3)
    came2 = lax.ppermute(after(part2, output_two), "tp", Z_DOWN)
    came3 = y_swap(after(there3, first_back[1]))
    second_back = attn_back(1, after(a1, here3, output_two))
    grad_heads.append(y_swap(second_back[1]))
    two_down = summed(info, after(part1, second_back[1]), came2, "all")
    came2 = lax.ppermute(two_down, "tp", Z_DOWN)
    back = [
        head_back(
            info,
            after(first_back[0], two_down),
            grad_heads[0],
            mine[0][1],
            theirs[0][1],
            *tables,
            heads,
        )
    ]
    part3 = summed(info, after(here3, back[0][0]), came3, "all", True)
    came3 = lax.ppermute(part3, "tp", Z_UP)
    back.append(
        head_back(
            info,
            after(second_back[0], part3),
            grad_heads[1],
            mine[1][1],
            theirs[1][1],
            *tables,
            heads,
        )
    )
    tokens_low, gain_one_sum = norm_one_back(
        info, [back[0][0], back[1][0]], proj_pieces, x_in, grad_resid, gain_one, 256
    )
    tokens_grad = spread(z_gather(tokens_low), F32)
    output_parts = [result_low, output_one, output_two, output_three]
    output = spread([after(part, tokens_low) for part in output_parts], BF16)

    def halves(v):
        half = v.shape[0] // 2
        return (
            lax.dynamic_slice_in_dim(v, ctx * half, half, 0),
            lax.dynamic_slice_in_dim(v, half - ctx * half, half, 0),
        )

    attn_parts = []
    for k in range(4):
        part = jnp.concatenate(
            [
                dot(normed_one_t, back[k % 2][0][k // 2], 1, 0).astype(BF16),
                dot(grad_attn_t, attended[k], 1, 0).astype(BF16),
            ],
            axis=1,
        )
        came = core_swap(part[width // 2 :])
        own = add_low(part[:quarter], came[:quarter])
        far = add_low(part[quarter : width // 2], came[quarter:])
        here, there = halves(add_low(own, x_swap(far)))
        attn_parts.append(add_low(here, y_swap(there)))

    here0, there0 = summed(info, after(own0, tokens_low), came0, "ctx")
    part0 = summed(info, here0, y_swap(there0), "all", True)

    def finish(own, turn):
        other = turn(y_swap(own))
        return jnp.concatenate(
            [jnp.where(ctx == 0, own, other), jnp.where(ctx == 0, other, own)], axis=0
        )

    ffn_sum = add(part0, came2) + came3.astype(F32)
    ffn_grad = finish(ffn_sum, turn_chunks)
    attn_grad = finish(z_reduce(attn_parts), lambda v: v)

    def total(v):
        for axis, pairs in (("fsdp", CORE_SWAP), ("fsdp", X_SWAP), ("ctx", Y_SWAP)):
            v = v + lax.ppermute(v, axis, pairs)
        for pairs in (Z_NEAR, Z_FAR):
            v = v + lax.ppermute(v, "tp", pairs)
        return v

    gain_heads = back[0][1] + back[1][1]
    sums = total(
        jnp.concatenate(
            [
                natural(gain_one_sum.reshape(4, quarter)).reshape(1, width),
                natural(gain_two_sum.reshape(4, quarter)).reshape(1, width),
                gain_heads[:, 0].reshape(1, hd),
                gain_heads[:, 1].reshape(1, hd),
                jnp.sum(square).reshape(1, 1),
                jnp.zeros((1, 127), F32),
            ],
            axis=1,
        )
    )[0]
    teacher_loss = sums[2 * width + 2 * hd] / (total_count * width)

    def own_part(at, size):
        return lax.dynamic_slice_in_dim(sums, at + fsdp * (size // 4), size // 4, 0)

    third = units // 3

    def columns(first):
        starts = [first(j) for j in range(3)]
        parts = [ffn_grad[:, s : s + third] for s in starts]
        return jnp.concatenate(
            [jnp.where(ctx == 0, parts[0], parts[2]), parts[1], jnp.where(ctx == 0, parts[2], parts[0])],
            axis=1,
        )

    return (
        output,
        teacher_loss,
        tokens_grad,
        own_part(0, width),
        attn_grad[:, :q_cols],
        attn_grad[:, q_cols : q_cols + k_cols],
        attn_grad[:, q_cols + k_cols : proj],
        own_part(2 * width, hd),
        own_part(2 * width + hd, hd),
        attn_grad[:, proj:].T,
        own_part(width, width),
        columns(lambda j: 2 * j * third),
        columns(lambda j: (2 * j + 1) * third),
        columns(lambda j: 2 * units + j * third).T,
    )


def solution(mesh):
    return jax.shard_map(
        per_device_rows if fits(mesh) else per_device_any,
        mesh=mesh,
        in_specs=(
            P("fsdp", "ctx", None),
            P("fsdp", "ctx", None),
            P("fsdp"),
            P("fsdp"),
            P("fsdp", "tp"),
            P("fsdp", "tp"),
            P("fsdp", "tp"),
            P("fsdp"),
            P("fsdp"),
            P("tp", "fsdp"),
            P("fsdp"),
            P("fsdp", "tp"),
            P("fsdp", "tp"),
            P("tp", "fsdp"),
        ),
        out_specs=(
            P("fsdp", "ctx", None),
            P(),
            P("fsdp", "ctx", None),
            P("fsdp"),
            P("fsdp", "tp"),
            P("fsdp", "tp"),
            P("fsdp", "tp"),
            P("fsdp"),
            P("fsdp"),
            P("tp", "fsdp"),
            P("fsdp"),
            P("fsdp", "tp"),
            P("fsdp", "tp"),
            P("tp", "fsdp"),
        ),
        check_vma=False,
    )
```

```python
import functools
import math

import jax
import jax.numpy as jnp
from jax import lax
from jax.experimental import pallas as pl
from jax.experimental.pallas import tpu as pltpu
from jax.sharding import PartitionSpec as P

EPS = 1e-05
THETA = 1000000.0
NEGATIVE = -1e30


def rms_scale(field_in, gain_vec):
    return (
        field_in * lax.rsqrt(jnp.mean(field_in * field_in, axis=-1, keepdims=True) + EPS) * gain_vec
    )


def rotate(field_in, positions):
    half_dim = field_in.shape[-1] // 2
    frequency = THETA ** (-(2.0 * jnp.arange(half_dim, dtype=jnp.float32)) / field_in.shape[-1])
    angles = positions[:, None] * frequency[None, :]
    cos_part = jnp.cos(angles)[:, None, :]
    sin_part = jnp.sin(angles)[:, None, :]
    lower_half = field_in[..., :half_dim]
    upper_half = field_in[..., half_dim:]
    return jnp.concatenate(
        [
            lower_half * cos_part - upper_half * sin_part,
            upper_half * cos_part + lower_half * sin_part,
        ],
        axis=-1,
    )


def linear(left_mat, right_mat):
    return jnp.dot(left_mat, right_mat, preferred_element_type=jnp.float32)


def linear_left(left_mat, right_mat):
    return lax.dot_general(
        left_mat, right_mat, (((0,), (0,)), ((), ())), preferred_element_type=jnp.float32
    )


def linear_right(left_mat, right_mat):
    return lax.dot_general(
        left_mat, right_mat, (((1,), (1,)), ((), ())), preferred_element_type=jnp.float32
    )


def swiglu(gate_act, up_act):
    return jax.nn.silu(gate_act) * up_act


def per_device_any(
    tokens,
    teacher,
    lengths,
    attn_gain,
    q_weight,
    k_weight,
    v_weight,
    q_gain,
    k_gain,
    o_weight,
    ffn_gain,
    gate_weight,
    up_weight,
    down_weight,
):
    (
        gain_one,
        w_query,
        w_key,
        w_value,
        gain_query,
        gain_key,
        w_output,
        gain_two,
        w_gate,
        w_upper,
        w_down,
    ) = (
        lax.all_gather(attn_gain, "fsdp", axis=0, tiled=True),
        lax.all_gather(q_weight, "fsdp", axis=0, tiled=True),
        lax.all_gather(k_weight, "fsdp", axis=0, tiled=True),
        lax.all_gather(v_weight, "fsdp", axis=0, tiled=True),
        lax.all_gather(q_gain, "fsdp", axis=0, tiled=True),
        lax.all_gather(k_gain, "fsdp", axis=0, tiled=True),
        lax.all_gather(o_weight, "fsdp", axis=1, tiled=True),
        lax.all_gather(ffn_gain, "fsdp", axis=0, tiled=True),
        lax.all_gather(gate_weight, "fsdp", axis=0, tiled=True),
        lax.all_gather(up_weight, "fsdp", axis=0, tiled=True),
        lax.all_gather(down_weight, "fsdp", axis=1, tiled=True),
    )
    rows_dev, block_len, model_width = tokens.shape
    count_tok = rows_dev * block_len
    head_dim = gain_query.shape[0]
    q_heads = w_query.shape[1] // head_dim
    kv_heads = w_key.shape[1] // head_dim
    group_size = q_heads // kv_heads
    score_scale = head_dim ** (-0.5)
    row_len = block_len * lax.axis_size("ctx")
    key_block = math.gcd(row_len, 512)
    block_start = lax.axis_index("ctx") * block_len
    tiles_used = (block_start + block_len + key_block - 1) // key_block
    slot_pos = block_start + jnp.arange(block_len, dtype=jnp.int32)
    positions = slot_pos.astype(jnp.float32)
    valid = (slot_pos[None, :] < lengths[:, None]).astype(jnp.float32)
    slots = count_tok * lax.axis_size("fsdp") * lax.axis_size("ctx")
    gain_two_f = gain_two.astype(jnp.float32)
    gain_one_f = gain_one.astype(jnp.float32)
    inputs = tokens.astype(jnp.float32)
    normed_one, back_one = jax.vjp(rms_scale, inputs, gain_one_f)
    normed_low = normed_one.astype(jnp.bfloat16).reshape(count_tok, model_width)
    query_raw = linear(normed_low, w_query)
    key_raw = linear(normed_low, w_key)
    value_raw = linear(normed_low, w_value)

    def heads_post(raw_heads, gain_vec):
        shaped = raw_heads.reshape(rows_dev, block_len, -1, head_dim)
        return rotate(rms_scale(shaped, gain_vec), positions)

    query_rot, query_back = jax.vjp(heads_post, query_raw, gain_query.astype(jnp.float32))
    key_rot, key_back = jax.vjp(heads_post, key_raw, gain_key.astype(jnp.float32))
    queries = query_rot.astype(jnp.bfloat16).reshape(
        rows_dev, block_len, kv_heads, group_size, head_dim
    )
    key_rows = key_rot.astype(jnp.bfloat16).reshape(rows_dev, block_len, kv_heads * head_dim)
    values = value_raw.astype(jnp.bfloat16).reshape(rows_dev, block_len, kv_heads * head_dim)
    keys_all, values_all = (
        lax.all_gather(key_rows, "ctx", axis=1, tiled=True),
        lax.all_gather(values, "ctx", axis=1, tiled=True),
    )

    def key_tile(tile_index):
        tile_start = tile_index * key_block
        key_pos = tile_start + jnp.arange(key_block, dtype=jnp.int32)
        key_part = lax.dynamic_slice_in_dim(keys_all, tile_start, key_block, 1).reshape(
            rows_dev, key_block, kv_heads, head_dim
        )
        value_part = lax.dynamic_slice_in_dim(values_all, tile_start, key_block, 1).reshape(
            rows_dev, key_block, kv_heads, head_dim
        )
        scores = (
            jnp.einsum("rqhgd,rkhd->rhgqk", queries, key_part, preferred_element_type=jnp.float32)
            * score_scale
        )
        allowed = (key_pos[None, None, :] <= slot_pos[None, :, None]) & (
            key_pos[None, None, :] < lengths[:, None, None]
        )
        return (tile_start, scores, allowed[:, None, None], key_part, value_part)

    stat_shape = (rows_dev, kv_heads, group_size, block_len)

    def stats_step(tile_index, carried):
        running_max, running_sum = carried
        tile_start, scores, allowed, key_part, value_part = key_tile(tile_index)
        masked = jnp.where(allowed, scores, NEGATIVE)
        new_max = jnp.maximum(running_max, jnp.max(masked, axis=-1))
        terms = jnp.where(allowed, jnp.exp(masked - new_max[..., None]), 0.0)
        return (new_max, running_sum * jnp.exp(running_max - new_max) + jnp.sum(terms, axis=-1))

    running_max, running_sum = lax.fori_loop(
        0,
        tiles_used,
        stats_step,
        (jnp.full(stat_shape, NEGATIVE, jnp.float32), jnp.zeros(stat_shape, jnp.float32)),
    )
    log_total = running_max + jnp.log(running_sum)
    out_shape = (rows_dev, block_len, kv_heads, group_size, head_dim)

    def value_step(tile_index, carried):
        rounded_out, exact_out = carried
        tile_start, scores, allowed, key_part, value_part = key_tile(tile_index)
        tile_probs = jnp.where(allowed, jnp.exp(scores - log_total[..., None]), 0.0)
        rounded_out = rounded_out + jnp.einsum(
            "rhgqk,rkhd->rqhgd",
            tile_probs.astype(jnp.bfloat16),
            value_part,
            preferred_element_type=jnp.float32,
        )
        exact_out = exact_out + jnp.einsum(
            "rhgqk,rkhd->rqhgd", tile_probs, value_part.astype(jnp.float32)
        )
        return (rounded_out, exact_out)

    rounded_out, exact_out = lax.fori_loop(
        0,
        tiles_used,
        value_step,
        (jnp.zeros(out_shape, jnp.float32), jnp.zeros(out_shape, jnp.float32)),
    )
    attended = rounded_out.astype(jnp.bfloat16).reshape(count_tok, q_heads * head_dim)
    attn_total = lax.psum(linear(attended, w_output), "tp")
    resid = inputs + attn_total.reshape(rows_dev, block_len, model_width)
    normed_two, back_two = jax.vjp(rms_scale, resid, gain_two_f)
    normed_second = normed_two.astype(jnp.bfloat16).reshape(count_tok, model_width)
    gate_act = linear(normed_second, w_gate)
    up_act = linear(normed_second, w_upper)
    hidden_full, back_glu = jax.vjp(swiglu, gate_act, up_act)
    hidden = hidden_full.astype(jnp.bfloat16)
    ffn_total = lax.psum(linear(hidden, w_down), "tp")
    result = resid + ffn_total.reshape(rows_dev, block_len, model_width)
    error_value = result - teacher.astype(jnp.float32)
    valid_col = valid[..., None]
    total_square, total_count = lax.psum(
        (jnp.sum(valid_col * error_value * error_value), jnp.sum(valid)), ("fsdp", "ctx")
    )
    teacher_loss = total_square / (total_count * model_width)
    grad_result = valid_col * error_value * (slots / total_count)
    grad_low = grad_result.astype(jnp.bfloat16).reshape(count_tok, model_width)
    grad_down = linear_left(hidden, grad_low)
    grad_hidden = linear_right(grad_low, w_down)
    grad_gate_full, grad_up_full = back_glu(grad_hidden)
    grad_gate = grad_gate_full.astype(jnp.bfloat16)
    grad_up = grad_up_full.astype(jnp.bfloat16)
    grad_wgate = linear_left(normed_second, grad_gate)
    grad_wup = linear_left(normed_second, grad_up)
    normed_two_part = linear_right(grad_gate, w_gate) + linear_right(grad_up, w_upper)
    grad_normed_two = lax.psum(normed_two_part, "tp")
    grad_resid_norm, grad_gain_two = back_two(
        grad_normed_two.reshape(rows_dev, block_len, model_width)
    )
    grad_resid = grad_result + grad_resid_norm
    grad_attn_low = grad_resid.astype(jnp.bfloat16).reshape(count_tok, model_width)
    grad_woutput = linear_left(attended, grad_attn_low)
    grad_attended = linear_right(grad_attn_low, w_output).astype(jnp.bfloat16).reshape(out_shape)
    delta = jnp.einsum("rqhgd,rqhgd->rhgq", grad_attended.astype(jnp.float32), exact_out)
    full_shape = (rows_dev, row_len, kv_heads * head_dim)

    def grad_step(tile_index, carried):
        grad_queries, grad_keys, grad_values = carried
        tile_start, scores, allowed, key_part, value_part = key_tile(tile_index)
        tile_probs = jnp.where(allowed, jnp.exp(scores - log_total[..., None]), 0.0)
        grad_probs = jnp.einsum(
            "rqhgd,rkhd->rhgqk", grad_attended, value_part, preferred_element_type=jnp.float32
        )
        grad_scores = (tile_probs * (grad_probs - delta[..., None])).astype(jnp.bfloat16)
        grad_queries = (
            grad_queries
            + jnp.einsum(
                "rhgqk,rkhd->rqhgd", grad_scores, key_part, preferred_element_type=jnp.float32
            )
            * score_scale
        )
        key_term = (
            jnp.einsum(
                "rhgqk,rqhgd->rkhd", grad_scores, queries, preferred_element_type=jnp.float32
            )
            * score_scale
        )
        value_term = jnp.einsum(
            "rhgqk,rqhgd->rkhd",
            tile_probs.astype(jnp.bfloat16),
            grad_attended,
            preferred_element_type=jnp.float32,
        )
        grad_keys = lax.dynamic_update_slice_in_dim(
            grad_keys, key_term.reshape(rows_dev, key_block, kv_heads * head_dim), tile_start, 1
        )
        grad_values = lax.dynamic_update_slice_in_dim(
            grad_values, value_term.reshape(rows_dev, key_block, kv_heads * head_dim), tile_start, 1
        )
        return (grad_queries, grad_keys, grad_values)

    grad_queries, grad_keys, grad_values = lax.fori_loop(
        0,
        tiles_used,
        grad_step,
        (
            jnp.zeros(out_shape, jnp.float32),
            jnp.zeros(full_shape, jnp.float32),
            jnp.zeros(full_shape, jnp.float32),
        ),
    )
    key_grad, value_grad = (
        lax.psum_scatter(grad_keys, "ctx", scatter_dimension=1, tiled=True),
        lax.psum_scatter(grad_values, "ctx", scatter_dimension=1, tiled=True),
    )
    grad_query_raw, grad_gain_query = query_back(
        grad_queries.reshape(rows_dev, block_len, q_heads, head_dim)
    )
    grad_key_raw, grad_gain_key = key_back(
        key_grad.reshape(rows_dev, block_len, kv_heads, head_dim)
    )
    query_low = grad_query_raw.astype(jnp.bfloat16)
    key_low = grad_key_raw.astype(jnp.bfloat16)
    value_low = value_grad.reshape(count_tok, kv_heads * head_dim).astype(jnp.bfloat16)
    grad_wquery = linear_left(normed_low, query_low)
    grad_wkey = linear_left(normed_low, key_low)
    grad_wvalue = linear_left(normed_low, value_low)
    normed_part = (
        linear_right(query_low, w_query)
        + linear_right(key_low, w_key)
        + linear_right(value_low, w_value)
    )
    grad_normed_one, grad_gain_query, grad_gain_key = lax.psum(
        (normed_part, grad_gain_query, grad_gain_key), "tp"
    )
    grad_input_norm, grad_gain_one = back_one(
        grad_normed_one.reshape(rows_dev, block_len, model_width)
    )
    tokens_grad = grad_resid + grad_input_norm
    partials = (
        grad_gain_one,
        grad_wquery,
        grad_wkey,
        grad_wvalue,
        grad_gain_query,
        grad_gain_key,
        grad_woutput,
        grad_gain_two,
        grad_wgate,
        grad_wup,
        grad_down,
    )
    pieces = (
        lax.psum_scatter(partials[0], ("fsdp", "ctx"), scatter_dimension=0, tiled=True),
        lax.psum_scatter(partials[1], ("fsdp", "ctx"), scatter_dimension=0, tiled=True),
        lax.psum_scatter(partials[2], ("fsdp", "ctx"), scatter_dimension=0, tiled=True),
        lax.psum_scatter(partials[3], ("fsdp", "ctx"), scatter_dimension=0, tiled=True),
        lax.psum_scatter(partials[4], ("fsdp", "ctx"), scatter_dimension=0, tiled=True),
        lax.psum_scatter(partials[5], ("fsdp", "ctx"), scatter_dimension=0, tiled=True),
        lax.psum_scatter(partials[6], ("fsdp", "ctx"), scatter_dimension=1, tiled=True),
        lax.psum_scatter(partials[7], ("fsdp", "ctx"), scatter_dimension=0, tiled=True),
        lax.psum_scatter(partials[8], ("fsdp", "ctx"), scatter_dimension=0, tiled=True),
        lax.psum_scatter(partials[9], ("fsdp", "ctx"), scatter_dimension=0, tiled=True),
        lax.psum_scatter(partials[10], ("fsdp", "ctx"), scatter_dimension=1, tiled=True),
    )
    summed = (
        lax.all_gather(pieces[0], "ctx", axis=0, tiled=True),
        lax.all_gather(pieces[1], "ctx", axis=0, tiled=True),
        lax.all_gather(pieces[2], "ctx", axis=0, tiled=True),
        lax.all_gather(pieces[3], "ctx", axis=0, tiled=True),
        lax.all_gather(pieces[4], "ctx", axis=0, tiled=True),
        lax.all_gather(pieces[5], "ctx", axis=0, tiled=True),
        lax.all_gather(pieces[6], "ctx", axis=1, tiled=True),
        lax.all_gather(pieces[7], "ctx", axis=0, tiled=True),
        lax.all_gather(pieces[8], "ctx", axis=0, tiled=True),
        lax.all_gather(pieces[9], "ctx", axis=0, tiled=True),
        lax.all_gather(pieces[10], "ctx", axis=1, tiled=True),
    )
    return (
        result.astype(jnp.bfloat16),
        teacher_loss,
        tokens_grad,
        summed[0],
        summed[1],
        summed[2],
        summed[3],
        summed[4],
        summed[5],
        summed[6],
        summed[7],
        summed[8],
        summed[9],
        summed[10],
    )


BF16 = jnp.bfloat16
F32 = jnp.float32
LOG2E = math.log2(math.e)
X_SWAP = [(0, 2), (2, 0), (1, 3), (3, 1)]
CORE_SWAP = [(0, 1), (1, 0), (2, 3), (3, 2)]
Y_SWAP = [(0, 1), (1, 0)]
Z_UP = [(0, 1), (1, 2), (2, 3), (3, 0)]
Z_DOWN = [(0, 3), (1, 0), (2, 1), (3, 2)]
Z_NEAR = [(0, 1), (1, 0), (2, 3), (3, 2)]
Z_FAR = [(0, 2), (2, 0), (1, 3), (3, 1)]
MASKS = (0, 2, 1, 3)
ANY = pl.BlockSpec(memory_space=pl.ANY)
SMEM = pl.BlockSpec(memory_space=pltpu.SMEM)


def fits(mesh):
    return dict(mesh.shape) == {"fsdp": 4, "ctx": 2, "tp": 4}


def dot(left, right, left_dim, right_dim):
    return lax.dot_general(
        left, right, (((left_dim,), (right_dim,)), ((), ())), preferred_element_type=F32
    )


def sigmoid(v):
    return 0.5 * jnp.tanh(0.5 * v) + 0.5


def whole(shape):
    zeros = (0,) * len(shape)
    return pl.BlockSpec(shape, lambda *_: zeros, pipeline_mode=pl.Buffered(1))


def settings(dims, mib):
    return pltpu.CompilerParams(
        dimension_semantics=("arbitrary",) * dims, vmem_limit_bytes=max(mib, 60) << 20
    )


def shape_of(shape, dtype):
    return jax.ShapeDtypeStruct(shape, dtype)


def cost(large):
    size = 1 << 42 if large else 1 << 10
    return pl.CostEstimate(flops=size, bytes_accessed=size >> 12, transcendentals=0)


def pack_kernel(info, o_in, g_in, u_in, d_in, out_ref, ffn_ref, o_ref, g_ref, u_ref, d_ref, sems):
    ctx = info[2]
    pairs = ((o_in, o_ref), (g_in, g_ref), (u_in, u_ref), (d_in, d_ref))
    copies = [pltpu.make_async_copy(a, b, sems.at[i]) for i, (a, b) in enumerate(pairs)]
    for copy in copies:
        copy.start()
    for copy in copies:
        copy.wait()
    out_ref[...] = o_ref[...].astype(F32).T.astype(BF16)
    third = g_ref.shape[1] // 3
    for j in range(3):
        at = pl.multiple_of(jnp.where(ctx == 0, j, 2 - j) * third, third)
        base = 3 * third * j
        ffn_ref[:, base : base + third] = g_ref[:, pl.ds(at, third)]
        ffn_ref[:, base + third : base + 2 * third] = u_ref[:, pl.ds(at, third)]
        down = d_ref[pl.ds(at, third), :].astype(F32).T.astype(BF16)
        ffn_ref[:, base + 2 * third : base + 3 * third] = down


def pack(info, o, g, u, d):
    rows = g.shape[0]
    return pl.pallas_call(
        pack_kernel,
        in_specs=[SMEM] + [ANY] * 4,
        out_specs=[pl.BlockSpec(memory_space=pltpu.VMEM)] * 2,
        out_shape=[shape_of((rows, o.shape[0]), BF16), shape_of((rows, 3 * g.shape[1]), BF16)],
        scratch_shapes=[pltpu.VMEM(a.shape, BF16) for a in (o, g, u, d)]
        + [pltpu.SemaphoreType.DMA((4,))],
        compiler_params=pltpu.CompilerParams(vmem_limit_bytes=60 << 20),
        cost_estimate=cost(False),
        name="pack",
    )(info, o, g, u, d)


def join_kernel(q_ref, k_ref, v_ref, out_ref, sems):
    at = 0
    copies = []
    for i, ref in enumerate((q_ref, k_ref, v_ref)):
        cols = pl.ds(at, ref.shape[1])
        copies.append(pltpu.make_async_copy(ref, out_ref.at[:, cols], sems.at[i]))
        copies[-1].start()
        at += ref.shape[1]
    for copy in copies:
        copy.wait()


def join(q, k, v):
    return pl.pallas_call(
        join_kernel,
        in_specs=[ANY] * 3,
        out_specs=ANY,
        out_shape=shape_of((q.shape[0], q.shape[1] + k.shape[1] + v.shape[1]), BF16),
        scratch_shapes=[pltpu.SemaphoreType.DMA((3,))],
        cost_estimate=cost(False),
        name="join",
    )(q, k, v)


def norm_one_kernel(info, tok_ref, gain_ref, x_ref, nt_ref, x32):
    quarter = x_ref.shape[1] // 4
    for p, mask in enumerate(MASKS):
        at = pl.multiple_of(jnp.bitwise_xor(info[1], mask) * quarter, quarter)
        part = tok_ref[0, :, pl.ds(at, quarter)]
        x_ref[:, p * quarter : (p + 1) * quarter] = part
        x32[:, p * quarter : (p + 1) * quarter] = part.astype(F32)
    x = x32[...]
    rho = lax.rsqrt(jnp.mean(x * x, axis=-1, keepdims=True) + EPS)
    nt_ref[...] = (x * rho * gain_ref[...]).T.astype(BF16)


def norm_one(info, tokens, gain, tile):
    _, tok, width = tokens.shape
    return pl.pallas_call(
        norm_one_kernel,
        grid_spec=pltpu.PrefetchScalarGridSpec(
            num_scalar_prefetch=1,
            grid=(tok // tile,),
            in_specs=[
                pl.BlockSpec((1, tile, width), lambda i, info: (info[0], i, 0)),
                pl.BlockSpec((1, width), lambda i, info: (0, 0)),
            ],
            out_specs=[
                pl.BlockSpec((tile, width), lambda i, info: (i, 0)),
                pl.BlockSpec((width, tile), lambda i, info: (0, i)),
            ],
            scratch_shapes=[pltpu.VMEM((tile, width), F32)],
        ),
        out_shape=[shape_of((tok, width), BF16), shape_of((width, tok), BF16)],
        compiler_params=settings(1, 24),
        cost_estimate=cost(False),
        name="norm_one",
    )(info, tokens, gain)


def proj_kernel(heads, block, info, *refs):
    pieces = [refs[4 * k : 4 * k + 4] for k in range(4)]
    nt_ref, cos_ref, sin_ref, qg_ref, kg_ref, rot_ref, raw_ref, w_ref, sem = refs[16:]
    rows = w_ref.shape[0] // 4

    @pl.when(pl.program_id(0) == 0)
    def _():
        for k in range(4):

            @pl.when(block(info) == k)
            def _():
                for p, piece in enumerate(pieces[k]):
                    pltpu.make_async_copy(piece, w_ref.at[pl.ds(p * rows, rows)], sem).start()

        pltpu.make_async_copy(w_ref, w_ref, sem).wait()

    hd = qg_ref.shape[0]
    half = hd // 2
    raw = dot(w_ref[...], nt_ref[...], 0, 0)
    cos_part, sin_part = cos_ref[...], sin_ref[...]
    heads_q, heads_k = heads
    raw_ref[...] = raw.astype(BF16)
    for h in range(heads_q + heads_k):
        v = raw[h * hd : (h + 1) * hd]
        rho = lax.rsqrt(jnp.mean(v * v, axis=0, keepdims=True) + EPS)
        v = v * rho * (qg_ref[...] if h < heads_q else kg_ref[...])
        a, b = v[:half], v[half:]
        rot_ref[h * hd : h * hd + half, :] = (a * cos_part - b * sin_part).astype(BF16)
        rot_ref[h * hd + half : (h + 1) * hd, :] = (b * cos_part + a * sin_part).astype(BF16)
    at = (heads_q + heads_k) * hd
    rot_ref[at:, :] = raw[at:].astype(BF16)


def project(info, pieces, normed_t, cos_part, sin_part, gain_q, gain_k, heads, block):
    width, tok = normed_t.shape
    cols = pieces[0][0].shape[1]
    tile = min(512, tok)
    const = lambda a: pl.BlockSpec(a.shape, lambda i, info: (0, 0))
    tab = lambda a: pl.BlockSpec((a.shape[0], tile), lambda i, info: (0, i))
    return pl.pallas_call(
        functools.partial(proj_kernel, heads, block),
        grid_spec=pltpu.PrefetchScalarGridSpec(
            num_scalar_prefetch=1,
            grid=(tok // tile,),
            in_specs=[ANY] * 16
            + [tab(normed_t), tab(cos_part), tab(sin_part), const(gain_q), const(gain_k)],
            out_specs=[pl.BlockSpec((cols, tile), lambda i, info: (0, i))] * 2,
            scratch_shapes=[pltpu.VMEM((width, cols), BF16), pltpu.SemaphoreType.DMA],
        ),
        out_shape=[shape_of((cols, tok), BF16), shape_of((cols, tok), BF16)],
        compiler_params=settings(1, 24),
        cost_estimate=cost(False),
        name="project",
    )(info, *[p for b in pieces for p in b], normed_t, cos_part, sin_part, gain_q, gain_k)


def head_back_kernel(
    heads, info, dm_ref, dt_ref, rm_ref, rt_ref, cos_ref, sin_ref, qg_ref, kg_ref, out_ref, gg_ref
):
    step, part = pl.program_id(0), pl.program_id(1)
    hd = qg_ref.shape[0]
    half = hd // 2
    heads_q, heads_k = heads
    cos_part, sin_part = cos_ref[...], sin_ref[...]
    tile = cos_part.shape[1]

    @pl.when((step == 0) & (part == 0))
    def _():
        gg_ref[...] = jnp.zeros_like(gg_ref)

    def work(d_ref, r_ref):
        gain_q = jnp.zeros((hd, 1), F32)
        gain_k = jnp.zeros((hd, 1), F32)
        done = []
        for h in range(heads_q + heads_k):
            is_q = h < heads_q
            g = d_ref[h * hd : (h + 1) * hd, :].astype(F32)
            raw = r_ref[h * hd : (h + 1) * hd, :].astype(F32)
            a, b = g[:half], g[half:]
            turned = jnp.concatenate(
                [a * cos_part + b * sin_part, b * cos_part - a * sin_part], axis=0
            )
            rho = lax.rsqrt(jnp.mean(raw * raw, axis=0, keepdims=True) + EPS)
            unit = raw * rho
            prod = turned * unit
            scaled = turned * (qg_ref[...] if is_q else kg_ref[...])
            mean = jnp.mean(scaled * unit, axis=0, keepdims=True)
            done.append(rho * (scaled - unit * mean))
            total = jnp.sum(prod, axis=1, keepdims=True)
            if is_q:
                gain_q = gain_q + total
            else:
                gain_k = gain_k + total
        done.append(d_ref[(heads_q + heads_k) * hd :, :].astype(F32))
        out_ref[0] = jnp.concatenate(done, axis=0).T.astype(BF16)
        lane = lax.broadcasted_iota(jnp.int32, gg_ref.shape, 1)
        gg_ref[...] += jnp.where(lane == 0, gain_q, jnp.where(lane == 1, gain_k, 0.0))

    @pl.when(step == 0)
    def _():
        work(dm_ref, rm_ref)

    @pl.when(step == 1)
    def _():
        work(dt_ref, rt_ref)


def head_back(info, grad_mine, grad_theirs, raw_mine, raw_theirs, cos_part, sin_part, gq, gk, heads):
    cols, tok = grad_mine.shape
    tile = min(512, tok)
    mine = pl.BlockSpec((cols, tile), lambda s, i, info: (0, jnp.where(s == 0, i, tok // tile - 1)))
    theirs = pl.BlockSpec((cols, tile), lambda s, i, info: (0, jnp.where(s == 0, 0, i)))
    tab = lambda a: pl.BlockSpec((a.shape[0], tile), lambda s, i, info: (0, i))
    const = lambda a: pl.BlockSpec(a.shape, lambda s, i, info: (0, 0))
    return pl.pallas_call(
        functools.partial(head_back_kernel, heads),
        grid_spec=pltpu.PrefetchScalarGridSpec(
            num_scalar_prefetch=1,
            grid=(2, tok // tile),
            in_specs=[
                mine,
                theirs,
                mine,
                theirs,
                tab(cos_part),
                tab(sin_part),
                const(gq),
                const(gk),
            ],
            out_specs=[
                pl.BlockSpec(
                    (1, tile, cols), lambda s, i, info: (jnp.bitwise_xor(info[2], s), i, 0)
                ),
                pl.BlockSpec((gq.shape[0], 128), lambda s, i, info: (0, 0)),
            ],
        ),
        out_shape=[shape_of((2, tok, cols), BF16), shape_of((gq.shape[0], 128), F32)],
        compiler_params=settings(2, 24),
        cost_estimate=cost(False),
        name="head_back",
    )(info, grad_mine, grad_theirs, raw_mine, raw_theirs, cos_part, sin_part, gq, gk)


def load_rows(info, mine_ref, got_ref, rows, sems):
    tok = mine_ref.shape[1]
    ctx = info[2]
    here = pl.multiple_of(ctx * tok, tok)
    there = pl.multiple_of((1 - ctx) * tok, tok)
    one = pltpu.make_async_copy(mine_ref, rows.at[:, pl.ds(here, tok)], sems.at[0])
    two = pltpu.make_async_copy(got_ref, rows.at[:, pl.ds(there, tok)], sems.at[1])
    one.start()
    two.start()
    one.wait()
    two.wait()


def keys_with_bias(keys, length):
    hd, slots = keys.shape
    pos = lax.broadcasted_iota(jnp.int32, (hd, slots), 1)
    row = lax.broadcasted_iota(jnp.int32, (hd, slots), 0)
    bias = jnp.where((row == 0) & (pos >= length), NEGATIVE, 0.0)
    return jnp.concatenate([keys.astype(F32), bias], axis=0).T.astype(BF16)


def query_with_one(pair):
    one_row = jnp.where(lax.broadcasted_iota(jnp.int32, pair.shape, 0) == 0, 1.0, 0.0)
    return jnp.concatenate([pair, one_row.astype(BF16)], axis=0)


def causal(scores, width):
    key_pos = lax.broadcasted_iota(jnp.int32, (width, width), 0)
    query_pos = lax.broadcasted_iota(jnp.int32, (width, width), 1)
    allowed = key_pos <= query_pos
    return jnp.where(jnp.concatenate([allowed, allowed], axis=1), scores, NEGATIVE)


def attn_fwd_kernel(
    width, hd, info, mine_ref, got_ref, keep_ref, send_ref, lse_ref, rows, key_rows, sems
):
    head, block = pl.program_id(0), pl.program_id(1)
    heads_k = pl.num_programs(0)
    scale = hd**-0.5 * LOG2E
    length = info[3]
    key_at = pl.multiple_of(heads_k * 2 * hd + head * hd, hd)
    value_at = pl.multiple_of(heads_k * 3 * hd + head * hd, hd)
    query_at = pl.multiple_of(head * 2 * hd, 2 * hd)

    @pl.when((head == 0) & (block == 0))
    def _():
        load_rows(info, mine_ref, got_ref, rows, sems)

    @pl.when(block == 0)
    def _():
        key_rows[...] = keys_with_bias(rows[pl.ds(key_at, hd), :], length)

    start = pl.multiple_of(block * width, width)
    both = rows[pl.ds(query_at, 2 * hd), pl.ds(start, width)]
    query = query_with_one(jnp.concatenate([both[:hd], both[hd:]], axis=1))

    def tile(at, carried, diagonal):
        out, total = carried
        scores = dot(key_rows[pl.ds(at, width), :], query, 1, 0)
        if diagonal:
            scores = causal(scores, width)
        probs = jnp.exp2(scores * scale)
        total = total + jnp.sum(probs, axis=0, keepdims=True)
        out = out + dot(rows[pl.ds(value_at, hd), pl.ds(at, width)], probs.astype(BF16), 1, 0)
        return out, total

    carried = (jnp.zeros((hd, 2 * width), F32), jnp.zeros((1, 2 * width), F32))
    full = jnp.minimum(block, lax.div(length + width - 1, width))
    carried = lax.fori_loop(
        0, full, lambda j, c: tile(pl.multiple_of(j * width, width), c, False), carried
    )
    out, total = tile(start, carried, True)
    out = out * (1.0 / total)
    out = jnp.concatenate([out[:, :width], out[:, width:]], axis=0).T.astype(BF16)
    here = block // 2 == info[2]

    @pl.when(here)
    def _():
        keep_ref[...] = out

    @pl.when(jnp.logical_not(here))
    def _():
        send_ref[...] = out

    log_total = jnp.log2(total)
    lse_ref[0, 0:1, :] = log_total[:, :width]
    lse_ref[0, 1:2, :] = log_total[:, width:]


def keep_block(i, info):
    return jnp.clip(i - 2 * info[2], 0, 1)


def send_block(i, info):
    return jnp.clip(i - 2 * (1 - info[2]), 0, 1)


def attn_fwd(info, mine, got, hd):
    cols, tok = mine.shape
    heads_k = cols // (4 * hd)
    width = tok // 2
    return pl.pallas_call(
        functools.partial(attn_fwd_kernel, width, hd),
        grid_spec=pltpu.PrefetchScalarGridSpec(
            num_scalar_prefetch=1,
            grid=(heads_k, 4),
            in_specs=[ANY, ANY],
            out_specs=[
                pl.BlockSpec((width, 2 * hd), lambda h, i, info: (keep_block(i, info), h)),
                pl.BlockSpec((width, 2 * hd), lambda h, i, info: (send_block(i, info), h)),
                pl.BlockSpec((1, 2, width), lambda h, i, info: (h, 0, i)),
            ],
            scratch_shapes=[
                pltpu.VMEM((cols, 2 * tok), BF16),
                pltpu.VMEM((2 * tok, 2 * hd), BF16),
                pltpu.SemaphoreType.DMA((2,)),
            ],
        ),
        out_shape=[
            shape_of((tok, heads_k * 2 * hd), BF16),
            shape_of((tok, heads_k * 2 * hd), BF16),
            shape_of((heads_k, 2, 2 * tok), F32),
        ],
        compiler_params=settings(2, 32),
        cost_estimate=cost(True),
        name="attn_fwd",
    )(info, mine, got)


def attn_bwd_kernel(
    width,
    hd,
    info,
    mine_ref,
    got_ref,
    ok_ref,
    os_ref,
    gk_ref,
    gs_ref,
    lse_ref,
    keep_ref,
    send_ref,
    rows,
    key_rows,
    value_rows,
    key_sum,
    value_sum,
    sems,
):
    head, block = pl.program_id(0), pl.program_id(1)
    heads_k = pl.num_programs(0)
    scale = hd**-0.5
    length = info[3]
    ctx = info[2]
    tok = keep_ref.shape[1]
    key_at = pl.multiple_of(heads_k * 2 * hd + head * hd, hd)
    value_at = pl.multiple_of(heads_k * 3 * hd + head * hd, hd)
    query_at = pl.multiple_of(head * 2 * hd, 2 * hd)

    @pl.when((head == 0) & (block == 0))
    def _():
        load_rows(info, mine_ref, got_ref, rows, sems)

    @pl.when(block == 0)
    def _():
        key_rows[...] = keys_with_bias(rows[pl.ds(key_at, hd), :], length)
        value_rows[...] = rows[pl.ds(value_at, hd), :].astype(F32).T.astype(BF16)
        key_sum[...] = jnp.zeros_like(key_sum)
        value_sum[...] = jnp.zeros_like(value_sum)

    start = pl.multiple_of(block * width, width)
    here = block // 2 == ctx

    def store_query(value):
        at = pl.ds(pl.multiple_of((block % 2) * width, width), width)

        @pl.when(here)
        def _():
            keep_ref[pl.ds(query_at, 2 * hd), at] = value

        @pl.when(jnp.logical_not(here))
        def _():
            send_ref[pl.ds(query_at, 2 * hd), at] = value

    @pl.when(block * width < length)
    def _():
        both = rows[pl.ds(query_at, 2 * hd), pl.ds(start, width)]
        pair = jnp.concatenate([both[:hd], both[hd:]], axis=1)
        query = query_with_one(pair)
        query_rows = pair.astype(F32).T.astype(BF16)
        grad_wide = jnp.where(here, gk_ref[...].astype(F32), gs_ref[...].astype(F32))
        out_wide = jnp.where(here, ok_ref[...].astype(F32), os_ref[...].astype(F32))
        grad_rows = jnp.concatenate([grad_wide[:, :hd], grad_wide[:, hd:]], axis=0).astype(BF16)
        grad_t = grad_wide.T
        prod = (grad_wide * out_wide).T
        grad = jnp.concatenate([grad_t[:hd], grad_t[hd:]], axis=1).astype(BF16)
        delta = jnp.concatenate(
            [
                jnp.sum(prod[:hd], axis=0, keepdims=True),
                jnp.sum(prod[hd:], axis=0, keepdims=True),
            ],
            axis=1,
        )
        lse = jnp.concatenate([lse_ref[0, 0:1, :], lse_ref[0, 1:2, :]], axis=1)

        def tile(at, query_sum, diagonal):
            scores = dot(key_rows[pl.ds(at, width), :], query, 1, 0)
            if diagonal:
                scores = causal(scores, width)
            probs = jnp.exp2(scores * (scale * LOG2E) - lse)
            grad_probs = dot(value_rows[pl.ds(at, width), :], grad, 1, 0)
            grad_scores = (probs * (grad_probs - delta)).astype(BF16)
            value_sum[pl.ds(at, width), :] += dot(probs.astype(BF16), grad_rows, 1, 0)
            key_sum[pl.ds(at, width), :] += dot(grad_scores, query_rows, 1, 0)
            return query_sum + dot(rows[pl.ds(key_at, hd), pl.ds(at, width)], grad_scores, 1, 0)

        query_sum = lax.fori_loop(
            0,
            block,
            lambda j, s: tile(pl.multiple_of(j * width, width), s, False),
            jnp.zeros((hd, 2 * width), F32),
        )
        query_sum = tile(start, query_sum, True) * scale
        store_query(
            jnp.concatenate([query_sum[:, :width], query_sum[:, width:]], axis=0).astype(BF16)
        )

    @pl.when(block * width >= length)
    def _():
        store_query(jnp.zeros((2 * hd, width), BF16))

    @pl.when(block == 3)
    def _():
        for at, total in ((key_at, key_sum[...] * scale), (value_at, value_sum[...])):
            total = total.T.astype(BF16)
            left, right = total[:, :tok], total[:, tok:]

            @pl.when(ctx == 0)
            def _():
                keep_ref[pl.ds(at, hd), :] = left
                send_ref[pl.ds(at, hd), :] = right

            @pl.when(ctx == 1)
            def _():
                keep_ref[pl.ds(at, hd), :] = right
                send_ref[pl.ds(at, hd), :] = left


def attn_bwd(info, mine, got, out_keep, out_send, grad_keep, grad_send, lse, hd):
    cols, tok = mine.shape
    heads_k = cols // (4 * hd)
    width = tok // 2
    keep = pl.BlockSpec((width, 2 * hd), lambda h, i, info: (keep_block(i, info), h))
    send = pl.BlockSpec((width, 2 * hd), lambda h, i, info: (send_block(i, info), h))
    full = pl.BlockSpec((cols, tok), lambda h, i, info: (0, 0))
    return pl.pallas_call(
        functools.partial(attn_bwd_kernel, width, hd),
        grid_spec=pltpu.PrefetchScalarGridSpec(
            num_scalar_prefetch=1,
            grid=(heads_k, 4),
            in_specs=[
                ANY,
                ANY,
                keep,
                send,
                keep,
                send,
                pl.BlockSpec((1, 2, width), lambda h, i, info: (h, 0, i)),
            ],
            out_specs=[full, full],
            scratch_shapes=[
                pltpu.VMEM((cols, 2 * tok), BF16),
                pltpu.VMEM((2 * tok, 2 * hd), BF16),
                pltpu.VMEM((2 * tok, hd), BF16),
                pltpu.VMEM((2 * tok, hd), F32),
                pltpu.VMEM((2 * tok, hd), F32),
                pltpu.SemaphoreType.DMA((2,)),
            ],
        ),
        out_shape=[shape_of((cols, tok), BF16), shape_of((cols, tok), BF16)],
        compiler_params=settings(2, 40),
        cost_estimate=cost(True),
        name="attn_bwd",
    )(info, mine, got, out_keep, out_send, grad_keep, grad_send, lse)


def load_blocks(pieces, target, sem):
    rows = target.shape[1] // 4

    @pl.when(pl.program_id(0) == 0)
    def _():
        for i, piece in enumerate(pieces):
            block = target.at[i // 4, pl.ds(i % 4 * rows, rows)]
            pltpu.make_async_copy(piece, block, sem).start()
        pltpu.make_async_copy(target, target, sem).wait()


def out_proj_kernel(info, *refs):
    x_ref, a0, a1, b0, b1, gain_ref, r_ref, n_ref, nt_ref, att_ref, w_ref, sem = refs[16:]
    load_blocks(refs[:16], w_ref, sem)
    ctx = info[2]
    total = x_ref[...].astype(F32)
    for j, ref, side in ((0, a0, ctx), (1, a1, ctx), (0, b0, 1 - ctx), (1, b1, 1 - ctx)):
        block = 2 * side + j
        part = ref[...]
        att_ref[block] = part
        total = total + dot(part, w_ref[block], 1, 1)
    rho = lax.rsqrt(jnp.mean(total * total, axis=-1, keepdims=True) + EPS)
    normed = total * rho * gain_ref[...]
    r_ref[...] = total
    n_ref[...] = normed.astype(BF16)
    nt_ref[...] = normed.T.astype(BF16)


def out_proj(info, x, mine, theirs, pieces, gain, tile):
    tok, width = x.shape
    feats = pieces[0][0].shape[1]
    rows_of = lambda n: pl.BlockSpec((tile, n), lambda i, info: (i, 0))
    return pl.pallas_call(
        out_proj_kernel,
        grid_spec=pltpu.PrefetchScalarGridSpec(
            num_scalar_prefetch=1,
            grid=(tok // tile,),
            in_specs=[ANY] * 16
            + [rows_of(width)]
            + [rows_of(feats)] * 4
            + [pl.BlockSpec((1, width), lambda i, info: (0, 0))],
            out_specs=[
                rows_of(width),
                rows_of(width),
                pl.BlockSpec((width, tile), lambda i, info: (0, i)),
                pl.BlockSpec((4, tile, feats), lambda i, info: (0, i, 0)),
            ],
            scratch_shapes=[pltpu.VMEM((4, width, feats), BF16), pltpu.SemaphoreType.DMA],
        ),
        out_shape=[
            shape_of((tok, width), F32),
            shape_of((tok, width), BF16),
            shape_of((width, tok), BF16),
            shape_of((4, tok, feats), BF16),
        ],
        compiler_params=settings(1, 32),
        cost_estimate=cost(True),
        name="out_proj",
    )(info, *[p for b in pieces for p in b], x, *mine, *theirs, gain)


def norm_two_back_kernel(info, *refs):
    g_ref, r_ref, gr_ref, gain_ref, gres_ref, gat_ref, a0, a1, b0, b1, gg_ref, w_ref, sem = refs[16:]
    load_blocks(refs[:16], w_ref, sem)
    ctx = info[2]
    grad, resid = g_ref[...], r_ref[...]
    rho = lax.rsqrt(jnp.mean(resid * resid, axis=-1, keepdims=True) + EPS)
    unit = resid * rho
    scaled = grad * gain_ref[...]
    back = rho * (scaled - unit * jnp.mean(scaled * unit, axis=-1, keepdims=True))
    total = gr_ref[...] + back
    gres_ref[...] = total
    low = total.astype(BF16)
    gat_ref[...] = total.T.astype(BF16)

    @pl.when(pl.program_id(0) == 0)
    def _():
        gg_ref[...] = jnp.zeros_like(gg_ref)

    gg_ref[...] += jnp.sum(grad * unit, axis=0, keepdims=True)
    for j, ref, side in ((0, a0, ctx), (1, a1, ctx), (0, b0, 1 - ctx), (1, b1, 1 - ctx)):
        ref[...] = dot(low, w_ref[2 * side + j], 1, 0).astype(BF16)


def norm_two_back(info, grad, resid, grad_result, gain, pieces, tile):
    tok, width = grad.shape
    feats = pieces[0][0].shape[1]
    rows_of = lambda n: pl.BlockSpec((tile, n), lambda i, info: (i, 0))
    row = pl.BlockSpec((1, width), lambda i, info: (0, 0))
    return pl.pallas_call(
        norm_two_back_kernel,
        grid_spec=pltpu.PrefetchScalarGridSpec(
            num_scalar_prefetch=1,
            grid=(tok // tile,),
            in_specs=[ANY] * 16 + [rows_of(width)] * 3 + [row],
            out_specs=[rows_of(width), pl.BlockSpec((width, tile), lambda i, info: (0, i))]
            + [rows_of(feats)] * 4
            + [row],
            scratch_shapes=[pltpu.VMEM((4, width, feats), BF16), pltpu.SemaphoreType.DMA],
        ),
        out_shape=[shape_of((tok, width), F32), shape_of((width, tok), BF16)]
        + [shape_of((tok, feats), BF16)] * 4
        + [shape_of((1, width), F32)],
        compiler_params=settings(1, 32),
        cost_estimate=cost(True),
        name="norm_two_back",
    )(info, *[p for b in pieces for p in b], grad, resid, grad_result, gain)


def norm_one_back_kernel(info, *refs):
    p0, p1, x_ref, gres_ref, gain_ref, outa_ref, outb_ref, gg_ref, w_ref, sem = refs[16:]
    load_blocks(refs[:16], w_ref, sem)
    quarter = x_ref.shape[1] // 4
    grad = dot(p0[0], w_ref[0], 1, 1)
    grad = grad + dot(p1[0], w_ref[1], 1, 1)
    grad = grad + dot(p0[1], w_ref[2], 1, 1)
    grad = grad + dot(p1[1], w_ref[3], 1, 1)
    x = x_ref[...].astype(F32)
    rho = lax.rsqrt(jnp.mean(x * x, axis=-1, keepdims=True) + EPS)
    unit = x * rho
    scaled = grad * gain_ref[...]
    back = rho * (scaled - unit * jnp.mean(scaled * unit, axis=-1, keepdims=True))
    total = (gres_ref[...] + back).astype(BF16)
    for p, mask in enumerate(MASKS):
        at = pl.multiple_of(jnp.bitwise_xor(info[1], mask) * quarter, quarter)
        part = total[:, p * quarter : (p + 1) * quarter]

        @pl.when(pl.program_id(0) < pl.num_programs(0) // 2)
        def _():
            outa_ref[:, pl.ds(at, quarter)] = part

        @pl.when(pl.program_id(0) >= pl.num_programs(0) // 2)
        def _():
            outb_ref[:, pl.ds(at, quarter)] = part

    @pl.when(pl.program_id(0) == 0)
    def _():
        gg_ref[...] = jnp.zeros_like(gg_ref)

    gg_ref[...] += jnp.sum(grad * unit, axis=0, keepdims=True)


def norm_one_back(info, pairs, pieces, x, grad_resid, gain, tile):
    tok, width = x.shape
    cols = pieces[0][0].shape[1]
    rows_of = lambda n: pl.BlockSpec((tile, n), lambda i, info: (i, 0))
    pair = pl.BlockSpec((2, tile, cols), lambda i, info: (0, i, 0))
    half = tok // tile // 2
    row = pl.BlockSpec((1, width), lambda i, info: (0, 0))
    return pl.pallas_call(
        norm_one_back_kernel,
        grid_spec=pltpu.PrefetchScalarGridSpec(
            num_scalar_prefetch=1,
            grid=(tok // tile,),
            in_specs=[ANY] * 16 + [pair, pair, rows_of(width), rows_of(width), row],
            out_specs=[
                pl.BlockSpec((tile, width), lambda i, info: (jnp.minimum(i, half - 1), 0)),
                pl.BlockSpec((tile, width), lambda i, info: (jnp.maximum(i - half, 0), 0)),
                row,
            ],
            scratch_shapes=[pltpu.VMEM((4, width, cols), BF16), pltpu.SemaphoreType.DMA],
        ),
        out_shape=[shape_of((tok // 2, width), BF16)] * 2 + [shape_of((1, width), F32)],
        compiler_params=settings(1, 32),
        cost_estimate=cost(True),
        name="norm_one_back",
    )(info, *[p for b in pieces for p in b], *pairs, x, grad_resid, gain)


def weight_copies(plan, pieces, gate_up, down, gate_up_sem, down_sem):
    third = down.shape[1] // 3
    rows = down.shape[0] // 4
    wide, thin = [], []
    for p, chunks in enumerate(plan):
        block = pl.ds(p * rows, rows)
        for j, (piece, at) in enumerate(chunks):
            src = pieces[piece]
            wide.append(
                pltpu.make_async_copy(
                    src.at[:, pl.ds(at, 2 * third)],
                    gate_up.at[block, pl.ds(j * 2 * third, 2 * third)],
                    gate_up_sem,
                )
            )
            thin.append(
                pltpu.make_async_copy(
                    src.at[:, pl.ds(at + 2 * third, third)],
                    down.at[block, pl.ds(j * third, third)],
                    down_sem,
                )
            )
    return wide, thin


def split_act(act):
    third = act.shape[1] // 6
    part = lambda j: act[:, j * third : (j + 1) * third]
    return [(part(0), part(1)), (part(2), part(3)), (part(4), part(5))]


def ffn_fwd_kernel(tile, plans, last, info, scale, x_ref, in_ref, *rest):
    if last:
        teach_ref, rest = rest[0], rest[1:]
    pieces = []
    for plan in plans:
        count = 1 + max(piece for chunks in plan for piece, _ in chunks)
        pieces.append(rest[:count])
        rest = rest[count:]
    act_ref, hid_ref = rest[:2]
    if last:
        outa_ref, outb_ref, gres_ref, low_ref, lowt_ref, sq_ref = rest[2:8]
        gate_up, down, total, sems = rest[8:]
    else:
        sum_ref, gate_up, down, total, sems = rest[2:]
    step, part = pl.program_id(0), pl.program_id(1)
    final = len(plans) - 1
    width = x_ref.shape[1]
    quarter = width // 4
    third = down.shape[2] // 3

    def copies(s):
        return weight_copies(
            plans[s], pieces[s], gate_up.at[s], down.at[s], sems.at[s, 0], sems.at[s, 1]
        )

    @pl.when((step == 0) & (part == 0))
    def _():
        for s in range(len(plans)):
            wide, thin = copies(s)
            for copy in wide + thin:
                copy.start()

    for s in range(len(plans)):

        @pl.when((step == s) & (part == 0))
        def _():
            pltpu.make_async_copy(gate_up.at[s], gate_up.at[s], sems.at[s, 0]).wait()
            pltpu.make_async_copy(down.at[s], down.at[s], sems.at[s, 1]).wait()

    rows = pl.ds(pl.multiple_of(part * tile, tile), tile)
    act = dot(x_ref[rows, :], gate_up[step], 1, 0)
    for j, (gate, upper) in enumerate(split_act(act)):
        hid_ref[0, :, j * third : (j + 1) * third] = (gate * sigmoid(gate) * upper).astype(BF16)
    act_ref[0] = act.astype(BF16)
    grown = dot(hid_ref[0], down[step], 1, 1)

    @pl.when(step == 0)
    def _():
        total[rows, :] = in_ref[...] + grown

    @pl.when(step > 0)
    def _():
        total[rows, :] += grown

    @pl.when(step == final)
    def _():
        result = total[rows, :]
        if not last:
            sum_ref[...] = result
            return
        tok = x_ref.shape[0]
        slot = info[2] * tok + part * tile + lax.broadcasted_iota(jnp.int32, (tile, 1), 0)
        valid = jnp.where(slot < info[3], 1.0, 0.0)
        square = jnp.zeros((tile, quarter), F32)
        for p, mask in enumerate(MASKS):
            at = pl.multiple_of(jnp.bitwise_xor(info[1], mask) * quarter, quarter)
            cols = slice(p * quarter, (p + 1) * quarter)
            value = result[:, cols]
            low = value.astype(BF16)

            @pl.when(part < pl.num_programs(1) // 2)
            def _():
                outa_ref[:, pl.ds(at, quarter)] = low

            @pl.when(part >= pl.num_programs(1) // 2)
            def _():
                outb_ref[:, pl.ds(at, quarter)] = low

            error = valid * (value - teach_ref[0, :, pl.ds(at, quarter)].astype(F32))
            square = square + error * error
            grad = error * scale[0]
            gres_ref[:, cols] = grad
            low_ref[:, cols] = grad.astype(BF16)
            lowt_ref[cols, :] = grad.T.astype(BF16)

        @pl.when(part == 0)
        def _():
            sq_ref[...] = jnp.zeros_like(sq_ref)

        sq_ref[...] += jnp.sum(square, axis=0, keepdims=True)


def ffn_fwd(info, scale, x, total, teacher, weights, units, tile):
    tok, width = x.shape
    pieces = [piece for _, group in weights for piece in group]
    count = len(weights)
    last = teacher is not None
    entry = lambda s, i: jnp.where(s == 0, i, tok // tile - 1)
    leave = lambda s, i: jnp.where(s == count - 1, i, 0)
    tiles = lambda n: pl.BlockSpec((tile, n), lambda s, i, info: (leave(s, i), 0))
    slab = lambda n: pl.BlockSpec((1, tile, n), lambda s, i, info: (s, i, 0))
    in_specs = [
        SMEM,
        whole((tok, width)),
        pl.BlockSpec((tile, width), lambda s, i, info: (entry(s, i), 0)),
    ]
    out_specs = [slab(2 * units), slab(units)]
    out_shape = [shape_of((count, tok, 2 * units), BF16), shape_of((count, tok, units), BF16)]
    if last:
        in_specs.append(
            pl.BlockSpec((1, tile, width), lambda s, i, info: (info[0], leave(s, i), 0))
        )
        half = tok // tile // 2
        out_specs += [
            pl.BlockSpec(
                (tile, width), lambda s, i, info: (jnp.minimum(leave(s, i), half - 1), 0)
            ),
            pl.BlockSpec(
                (tile, width), lambda s, i, info: (jnp.maximum(leave(s, i) - half, 0), 0)
            ),
            tiles(width),
            tiles(width),
            pl.BlockSpec((width, tile), lambda s, i, info: (0, leave(s, i))),
            pl.BlockSpec((1, width // 4), lambda s, i, info: (0, 0)),
        ]
        out_shape += [
            shape_of((tok // 2, width), BF16),
            shape_of((tok // 2, width), BF16),
            shape_of((tok, width), F32),
            shape_of((tok, width), BF16),
            shape_of((width, tok), BF16),
            shape_of((1, width // 4), F32),
        ]
    else:
        out_specs.append(tiles(width))
        out_shape.append(shape_of((tok, width), F32))
    return pl.pallas_call(
        functools.partial(ffn_fwd_kernel, tile, [plan for plan, _ in weights], last),
        grid_spec=pltpu.PrefetchScalarGridSpec(
            num_scalar_prefetch=1,
            grid=(count, tok // tile),
            in_specs=in_specs + [ANY] * len(pieces),
            out_specs=out_specs,
            scratch_shapes=[
                pltpu.VMEM((count, width, 2 * units), BF16),
                pltpu.VMEM((count, width, units), BF16),
                pltpu.VMEM((tok, width), F32),
                pltpu.SemaphoreType.DMA((count, 2)),
            ],
        ),
        out_shape=out_shape,
        compiler_params=settings(2, 50),
        cost_estimate=cost(True),
        name="ffn_fwd",
    )(info, scale, x, total, *([teacher] if last else []), *pieces)


def ffn_bwd_kernel(steps, plan, first, low_ref, act_ref, hid_ref, xt_ref, lowt_ref, *rest):
    count = 1 + max(piece for chunks in plan for piece, _ in chunks)
    pieces, rest = rest[:count], rest[count:]
    if not first:
        in_ref, rest = rest[0], rest[1:]
    out_ref, keep_ref, send_ref, gate_up, down, dact_all, hid_all, sems = rest
    step = pl.program_id(0)
    units = down.shape[1]
    third = units // 3
    tile = low_ref.shape[0]

    @pl.when(step == 0)
    def _():
        wide, thin = weight_copies(plan, pieces, gate_up, down, sems.at[0], sems.at[1])
        for copy in thin + wide:
            copy.start()
        pltpu.make_async_copy(down, down, sems.at[1]).wait()

    @pl.when(step < steps)
    def _():
        rows = pl.ds(pl.multiple_of(step * tile, tile), tile)
        grad_hidden = dot(low_ref[...], down[...], 1, 0)
        for j, (gate, upper) in enumerate(split_act(act_ref[0])):
            grad = grad_hidden[:, j * third : (j + 1) * third]
            gate, upper = gate.astype(F32), upper.astype(F32)
            sig = sigmoid(gate)
            silu = gate * sig
            at = 2 * j * third
            dact_all[rows, at : at + third] = (
                grad * upper * (sig + silu - silu * sig)
            ).astype(BF16)
            dact_all[rows, at + third : at + 2 * third] = (grad * silu).astype(BF16)
        hid_all[rows, :] = hid_ref[0]

        @pl.when(step == 0)
        def _():
            pltpu.make_async_copy(gate_up, gate_up, sems.at[0]).wait()

        grown = dot(dact_all[rows, :], gate_up[...], 1, 1)
        out_ref[...] = grown if first else in_ref[...] + grown

    def weight_rows(target):
        target[:, : 2 * units] = dot(xt_ref[...], dact_all[...], 1, 0).astype(BF16)
        target[:, 2 * units :] = dot(lowt_ref[...], hid_all[...], 1, 0).astype(BF16)

    @pl.when((step >= steps) & (step < steps + 2))
    def _():
        weight_rows(send_ref)

    @pl.when(step >= steps + 2)
    def _():
        weight_rows(keep_ref)


def ffn_bwd(low, saved, weights, total, xt, lowt, tile):
    plan, pieces = weights
    acts, hiddens, block = saved
    tok, width = low.shape
    units = hiddens.shape[2]
    steps = tok // tile
    quarter = width // 4
    first = total is None
    clip = lambda i: jnp.minimum(i, steps - 1)
    rows_of = lambda n: pl.BlockSpec((tile, n), lambda i: (clip(i), 0))
    slab = lambda n: pl.BlockSpec((1, tile, n), lambda i: (block, clip(i), 0))
    feature = lambda i: (jnp.where(i < steps + 2, jnp.maximum(i - steps, 0) + 2, i - steps - 2), 0)
    return pl.pallas_call(
        functools.partial(ffn_bwd_kernel, steps, plan, first),
        grid=(steps + 4,),
        in_specs=[
            rows_of(width),
            slab(2 * units),
            slab(units),
            pl.BlockSpec((quarter, tok), feature),
            pl.BlockSpec((quarter, tok), feature),
        ]
        + [ANY] * len(pieces)
        + ([] if first else [rows_of(width)]),
        out_specs=[
            rows_of(width),
            pl.BlockSpec((quarter, 3 * units), lambda i: (jnp.maximum(i - steps - 2, 0), 0)),
            pl.BlockSpec((quarter, 3 * units), lambda i: (jnp.clip(i - steps, 0, 1), 0)),
        ],
        out_shape=[
            shape_of((tok, width), F32),
            shape_of((width // 2, 3 * units), BF16),
            shape_of((width // 2, 3 * units), BF16),
        ],
        scratch_shapes=[
            pltpu.VMEM((width, 2 * units), BF16),
            pltpu.VMEM((width, units), BF16),
            pltpu.VMEM((tok, 2 * units), BF16),
            pltpu.VMEM((tok, units), BF16),
            pltpu.SemaphoreType.DMA((2,)),
        ],
        input_output_aliases={} if first else {5 + len(pieces): 0},
        compiler_params=settings(1, 56),
        cost_estimate=cost(True),
        name="ffn_bwd",
    )(low, acts, hiddens, xt, lowt, *pieces, *([] if first else [total]))


def turn_chunks(block):
    wide = block.shape[1] * 2 // 9
    thin = wide // 2
    starts = [(2 * wide, wide), (wide, wide), (0, wide)]
    starts += [(3 * wide + 2 * thin, thin), (3 * wide + thin, thin), (3 * wide, thin)]
    return jnp.concatenate([block[:, a : a + n] for a, n in starts], axis=1)


def sum_kernel(turns, *refs):
    total = None
    for ref, turn in zip(refs[:-1], turns):
        value = ref[...].astype(F32)
        value = turn_chunks(value) if turn else value
        total = value if total is None else total + value
    refs[-1][...] = total.astype(refs[-1].dtype)


def summed(terms, turns=None, dtype=BF16):
    rows, cols = terms[0].shape
    spec = pl.BlockSpec((64, cols), lambda i: (i, 0))
    return pl.pallas_call(
        functools.partial(sum_kernel, turns or [False] * len(terms)),
        grid=(rows // 64,),
        in_specs=[spec] * len(terms),
        out_specs=spec,
        out_shape=shape_of((rows, cols), dtype),
        compiler_params=settings(1, 24),
        cost_estimate=cost(False),
        name="summed",
    )(*terms)


def core_sum_kernel(info, left_ref, right_ref, *outs):
    total = (left_ref[...].astype(F32) + right_ref[...].astype(F32)).astype(BF16)
    block = pl.program_id(0) // 2
    far, other = block // 2, jnp.bitwise_xor(block % 2, info[2])
    for i, out in enumerate(outs):

        @pl.when(far * 2 + other == i)
        def _():
            out[...] = total


def core_sum(info, keep, came):
    rows, cols = keep.shape
    block = lambda at: pl.BlockSpec((64, cols), at)

    def place(far, other):
        def at(i, info):
            return (jnp.clip(i - 4 * far - 2 * jnp.bitwise_xor(info[2], other), 0, 1), 0)

        return block(at)

    return pl.pallas_call(
        core_sum_kernel,
        grid_spec=pltpu.PrefetchScalarGridSpec(
            num_scalar_prefetch=1,
            grid=(rows // 64,),
            in_specs=[block(lambda i, info: (i, 0))] * 2,
            out_specs=[place(0, 0), place(0, 1), place(1, 0), place(1, 1)],
        ),
        out_shape=[shape_of((rows // 4, cols), BF16)] * 4,
        compiler_params=settings(1, 24),
        cost_estimate=cost(False),
        name="core_sum",
    )(info, keep, came)


def weight_grad_kernel(nt_ref, back_ref, gt_ref, att_ref, keep_ref, send_ref):
    cols = back_ref.shape[2]

    def rows(target):
        target[:, :cols] = dot(nt_ref[...], back_ref[0], 1, 0).astype(BF16)
        target[:, cols:] = dot(gt_ref[...], att_ref[0], 1, 0).astype(BF16)

    @pl.when(pl.program_id(0) < 2)
    def _():
        rows(send_ref)

    @pl.when(pl.program_id(0) >= 2)
    def _():
        rows(keep_ref)


def weight_grad(normed_t, back, side, grad_t, attended, block):
    width, tok = normed_t.shape
    cols, feats = back.shape[2], attended.shape[2]
    rows = pl.BlockSpec((width // 4, tok), lambda i: (jnp.bitwise_xor(i, 2), 0))
    return pl.pallas_call(
        weight_grad_kernel,
        grid=(4,),
        in_specs=[
            rows,
            pl.BlockSpec((1, tok, cols), lambda i: (side, 0, 0)),
            rows,
            pl.BlockSpec((1, tok, feats), lambda i: (block, 0, 0)),
        ],
        out_specs=[
            pl.BlockSpec((width // 4, cols + feats), lambda i: (jnp.maximum(i - 2, 0), 0)),
            pl.BlockSpec((width // 4, cols + feats), lambda i: (jnp.minimum(i, 1), 0)),
        ],
        out_shape=[shape_of((width // 2, cols + feats), BF16)] * 2,
        compiler_params=settings(1, 24),
        cost_estimate=cost(False),
        name="weight_grad",
    )(normed_t, back, grad_t, attended)


def after(value, *others):
    return lax.optimization_barrier((value,) + others)[0]


def per_device_rows(
    tokens,
    teacher,
    lengths,
    attn_gain,
    q_weight,
    k_weight,
    v_weight,
    q_gain,
    k_gain,
    o_weight,
    ffn_gain,
    gate_weight,
    up_weight,
    down_weight,
):
    z = lax.axis_index("tp")
    ctx = lax.axis_index("ctx")
    fsdp = lax.axis_index("fsdp")
    rows_dev, tok, width = tokens.shape
    quarter = width // 4
    hd = q_gain.shape[0] * 4
    q_cols, k_cols = q_weight.shape[1], k_weight.shape[1]
    proj = q_cols + 2 * k_cols
    heads = (q_cols // hd, k_cols // hd)
    units = gate_weight.shape[1]
    slots = rows_dev * 4 * tok * 2

    def x_swap(v):
        return lax.ppermute(v, "fsdp", X_SWAP)

    def core_swap(v):
        return lax.ppermute(v, "fsdp", CORE_SWAP)

    def y_swap(v):
        return lax.ppermute(v, "ctx", Y_SWAP)

    def z_up(v):
        return lax.ppermute(v, "tp", Z_UP)

    def z_far(v):
        return lax.ppermute(v, "tp", Z_FAR)

    def z_down(v):
        return lax.ppermute(v, "tp", Z_DOWN)

    def chunks(block):
        return [block[:, j * units : (j + 1) * units] for j in range(3)]

    def natural(v):
        v = jnp.concatenate([v[0:1], v[2:3], v[1:2], v[3:4]], axis=0)
        v = jnp.where(fsdp % 2 == 0, v, jnp.concatenate([v[1:2], v[0:1], v[3:4], v[2:3]], axis=0))
        return jnp.where(fsdp // 2 == 0, v, jnp.concatenate([v[2:4], v[0:2]], axis=0))

    v = {}

    def sync():
        v.update(lax.optimization_barrier(dict(v)))

    length = lax.dynamic_slice_in_dim(lengths, z, 1, 0)
    info = jnp.concatenate([jnp.stack([z, fsdp, ctx]).astype(jnp.int32), length])
    w_proj = join(q_weight, k_weight, v_weight)
    proj_blocks = [w_proj, z_up(w_proj), z_far(w_proj), z_down(w_proj)]
    proj_far = [x_swap(w_proj)]
    w_out, w_ffn = pack(info, o_weight, gate_weight, up_weight, down_weight)
    count_here = jnp.sum(lengths).astype(F32)[None]
    vector = jnp.concatenate([attn_gain, ffn_gain, q_gain, k_gain]).astype(F32)
    vector = jnp.concatenate([vector, count_here, jnp.zeros((640 - 545,), F32)])[None]
    vector = jnp.concatenate([vector, x_swap(vector)], axis=0)
    pos = (ctx * tok + jnp.arange(tok, dtype=jnp.int32)).astype(F32)
    frequency = THETA ** (-(2.0 * jnp.arange(hd // 2, dtype=F32)) / hd)
    angles = frequency[:, None] * pos[None, :]
    v.update(
        info=info,
        proj_blocks=proj_blocks,
        proj_far=proj_far,
        w_out=w_out,
        w_ffn=w_ffn,
        vector=vector,
        cos_part=jnp.cos(angles),
        sin_part=jnp.sin(angles),
    )
    sync()
    info = v["info"]

    proj_far = v["proj_far"] + [x_swap(block) for block in v["proj_blocks"][1:]]
    w_out = v["w_out"]
    out_blocks = [w_out, z_up(w_out), z_far(w_out), z_down(w_out)]
    own_cores = [core_swap(v["proj_blocks"][0]), core_swap(proj_far[0])]
    vector = jnp.concatenate([v["vector"], core_swap(v["vector"])], axis=0)
    gain_one = vector[:, :quarter].reshape(1, width)
    gain_two = vector[:, quarter : 2 * quarter].reshape(1, width)
    total_count = jnp.sum(vector[:, 544])
    head_gains = natural(vector[:, 2 * quarter : 544])
    x_in, normed_one_t = norm_one(info, tokens, gain_one, 256)
    v.update(
        proj_far=proj_far,
        out_blocks=out_blocks,
        own_cores=own_cores,
        gain_one=gain_one,
        gain_two=gain_two,
        gain_q=head_gains[:, : hd // 4].reshape(hd, 1),
        gain_k=head_gains[:, hd // 4 :].reshape(hd, 1),
        total_count=total_count,
        x_in=x_in,
        normed_one_t=normed_one_t,
    )
    sync()

    ffn_one = z_up(v["w_ffn"])
    ffn_far = x_swap(v["w_ffn"])
    proj_pieces = []
    for k, (block, far) in enumerate(zip(v["proj_blocks"], v["proj_far"])):
        cores = v["own_cores"] if k == 0 else [core_swap(block), core_swap(far)]
        proj_pieces.append([block, far] + cores)
    tables = [v[name] for name in ("cos_part", "sin_part", "gain_q", "gain_k")]

    def make(block, *then):
        return project(info, proj_pieces, after(v["normed_one_t"], *then), *tables, heads, block)

    theirs = [make(lambda s: 2 * (1 - s[2]))]
    got = [y_swap(theirs[0][0])]
    theirs.append(make(lambda s: 2 * (1 - s[2]) + 1, theirs[0][0]))
    got.append(y_swap(theirs[1][0]))
    mine = [make(lambda s: 2 * s[2], theirs[1][0])]
    mine.append(make(lambda s: 2 * s[2] + 1, mine[0][0]))
    v.update(
        ffn_one=ffn_one,
        ffn_far=ffn_far,
        proj_pieces=proj_pieces,
        mine=mine,
        theirs=theirs,
        got0=got[0],
    )
    sync()

    one_far = [x_swap(chunks(v["ffn_one"])[0])]
    three = [z_down(chunks(v["w_ffn"])[0])]
    first = attn_fwd(info, v["mine"][0][0], v["got0"], hd)
    v.update(first=first, got1=got[1], one_far=one_far, three=three)
    sync()

    arrived = [y_swap(v["first"][1])]
    three = v["three"] + [z_down(chunks(v["w_ffn"])[1])]
    out_far = [x_swap(block) for block in v["out_blocks"]]
    own_cores = [core_swap(v["w_ffn"]), core_swap(v["ffn_far"])]
    second = attn_fwd(info, v["mine"][1][0], v["got1"], hd)
    v.update(
        second=second, arrived=arrived, three=three, out_far=out_far, own_cores=own_cores
    )
    sync()

    arrived = v["arrived"] + [y_swap(v["second"][1])]
    three = v["three"] + [z_down(chunks(v["w_ffn"])[2])]
    one_far = v["one_far"] + [x_swap(chunks(v["ffn_one"])[1])]
    one_cores = [core_swap(v["ffn_one"]), core_swap(one_far[0])]
    out_pieces = [
        [block, far, core_swap(block), core_swap(far)]
        for block, far in zip(v["out_blocks"], v["out_far"])
    ]
    v.update(
        arrived=arrived, three=three, one_far=one_far, one_cores=one_cores, out_pieces=out_pieces
    )
    sync()

    two = [z_up(chunks(v["ffn_one"])[0])]
    three_far = [x_swap(v["three"][0])]
    one_last = y_swap(v["one_far"][0])
    one_cores = v["one_cores"] + [core_swap(v["one_far"][1])]
    three_cores = [core_swap(v["three"][0]), core_swap(v["three"][1])]
    resid, normed_two, normed_two_t, attended = out_proj(
        info,
        v["x_in"],
        [v["first"][0], v["second"][0]],
        v["arrived"],
        v["out_pieces"],
        v["gain_two"],
        256,
    )
    v.update(
        two=two,
        three_far=three_far,
        one_last=one_last,
        one_cores=one_cores,
        three_cores=three_cores,
        resid=resid,
        normed_two=normed_two,
        normed_two_t=normed_two_t,
        attended=attended,
    )
    sync()

    in_block = lambda i: [(i, 0), (i, units), (i, 2 * units)]
    in_row = lambda i: [(i, 0), (i + 1, 0), (i + 2, 0)]
    plan0 = [in_block(i) for i in range(4)]
    plan1 = [in_block(0), in_row(1), in_block(4), in_row(5)]
    plan3 = [in_row(3 * i) for i in range(4)]
    scale = (slots / v["total_count"])[None]
    weights0 = [v["w_ffn"], v["ffn_far"]] + v["own_cores"]
    weights1 = [v["ffn_one"]] + v["one_far"] + [v["one_last"]]
    weights1 += v["one_cores"] + [core_swap(v["one_last"])]
    two = v["two"] + [z_up(part) for part in chunks(v["ffn_one"])[1:]]
    three_far = v["three_far"] + [x_swap(v["three"][1])]
    two_far = [x_swap(v["two"][0])]
    three_last = y_swap(v["three_far"][0])
    three_cores = v["three_cores"] + [core_swap(v["three"][2]), core_swap(v["three_far"][0])]
    two_cores = [core_swap(v["two"][0])]
    acts_a, hiddens_a, sum_a = ffn_fwd(
        info,
        scale,
        v["normed_two"],
        v["resid"],
        None,
        [(plan0, weights0), (plan1, weights1)],
        units,
        256,
    )
    v.update(
        scale=scale,
        weights0=weights0,
        weights1=weights1,
        two=two,
        three_far=three_far,
        two_far=two_far,
        three_last=three_last,
        three_cores=three_cores,
        two_cores=two_cores,
        acts_a=acts_a,
        hiddens_a=hiddens_a,
        sum_a=sum_a,
    )
    sync()

    weights3 = v["three"] + v["three_far"] + [v["three_last"]] + v["three_cores"]
    weights3 += [core_swap(v["three_far"][1]), core_swap(v["three_last"])]
    two_far = v["two_far"] + [x_swap(v["two"][1])]
    two_last = y_swap(v["two_far"][0])
    two_cores = v["two_cores"] + [core_swap(p) for p in v["two"][1:] + v["two_far"]]
    acts_b, hiddens_b, sum_b = ffn_fwd(
        info, v["scale"], v["normed_two"], v["sum_a"], None, [(plan3, weights3)], units, 256
    )
    v.update(
        weights3=weights3,
        two_far=two_far,
        two_last=two_last,
        two_cores=two_cores,
        acts_b=acts_b,
        hiddens_b=hiddens_b,
        sum_b=sum_b,
    )
    sync()

    weights2 = v["two"] + v["two_far"] + [v["two_last"]] + v["two_cores"]
    weights2 += [core_swap(v["two_far"][1]), core_swap(v["two_last"])]
    acts_c, hiddens_c, *results, grad_result, grad_low, grad_low_t, square = ffn_fwd(
        info, v["scale"], v["normed_two"], v["sum_b"], teacher, [(plan3, weights2)], units, 256
    )
    v.update(
        weights2=weights2,
        acts_c=acts_c,
        hiddens_c=hiddens_c,
        results=results,
        grad_result=grad_result,
        grad_low=grad_low,
        grad_low_t=grad_low_t,
        square=square,
    )
    sync()

    def ffn_back(plan, weights, acts, hiddens, block, total):
        return ffn_bwd(
            v["grad_low"],
            (v[acts], v[hiddens], block),
            (plan, v[weights]),
            total,
            v["normed_two_t"],
            v["grad_low_t"],
            256,
        )

    turned = [False, False, True]
    one = [z_up(v["results"][0])]
    total, keep2, send2 = ffn_back(plan3, "weights2", "acts_c", "hiddens_c", 0, None)
    v.update(one=one, total=total, keep2=keep2, send2=send2)
    sync()

    one = v["one"] + [z_up(v["results"][1])]
    came2 = core_swap(v["send2"])
    total, keep1, send1 = ffn_back(plan1, "weights1", "acts_a", "hiddens_a", 1, v["total"])
    v.update(one=one, came2=came2, total=total, keep1=keep1, send1=send1)
    sync()

    out_three = [z_down(v["results"][0])]
    came1 = core_swap(v["send1"])
    sum2 = core_sum(info, v["keep2"], v["came2"])
    far_t2 = x_swap(sum2[3])
    total, keep3, send3 = ffn_back(
        plan3, "weights3", "acts_b", "hiddens_b", 0, after(v["total"], sum2[0])
    )
    v.update(
        out_three=out_three,
        came1=came1,
        sum2=sum2,
        far_t2=far_t2,
        total=total,
        keep3=keep3,
        send3=send3,
    )
    sync()

    out_three = v["out_three"] + [z_down(v["results"][1])]
    came3 = core_swap(v["send3"])
    far_h2 = x_swap(v["sum2"][2])
    there2 = y_swap(summed([v["sum2"][1], v["far_t2"]]))
    sum1 = core_sum(info, v["keep1"], v["came1"])
    total, keep0, send0 = ffn_back(
        plan0, "weights0", "acts_a", "hiddens_a", 0, after(v["total"], sum1[0])
    )
    v.update(
        out_three=out_three,
        came3=came3,
        far_h2=far_h2,
        there2=there2,
        sum1=sum1,
        total=total,
        keep0=keep0,
        send0=send0,
    )
    sync()

    came0 = core_swap(v["send0"])
    far_t1 = x_swap(v["sum1"][3])
    down2 = z_down(summed([v["sum2"][0], v["far_h2"], v["there2"]], turned))
    sum3 = core_sum(info, v["keep3"], v["came3"])
    grad_resid, grad_attn_t, a0, a1, b0, b1, gain_two_sum = norm_two_back(
        info,
        after(v["total"], sum3[0]),
        v["resid"],
        v["grad_result"],
        v["gain_two"],
        v["out_pieces"],
        256,
    )
    grad_got = [y_swap(b0), y_swap(b1)]
    v.update(
        came0=came0,
        far_t1=far_t1,
        down2=down2,
        sum3=sum3,
        grad_resid=grad_resid,
        grad_attn_t=grad_attn_t,
        grad_mine=[a0, a1],
        gain_two_sum=gain_two_sum,
        grad_got0=grad_got[0],
    )
    sync()

    def attn_back(j, grad):
        out, got_ref = v["first" if j == 0 else "second"], v[f"got{j}"]
        return attn_bwd(
            info, v["mine"][j][0], got_ref, out[0], out[1], grad, v[f"grad_got{j}"], out[2], hd
        )

    two = [z_up(v["one"][0])]
    far_h1 = x_swap(v["sum1"][2])
    there1 = y_swap(summed([v["sum1"][1], v["far_t1"]]))
    far_t3 = x_swap(v["sum3"][3])
    sum0 = core_sum(info, v["keep0"], v["came0"])
    back0 = attn_back(0, after(v["grad_mine"][0], sum0[0], there1))
    v.update(
        out_two=two,
        far_h1=far_h1,
        there1=there1,
        far_t3=far_t3,
        sum0=sum0,
        back0=back0,
        grad_got1=grad_got[1],
    )
    sync()

    two = v["out_two"] + [z_up(v["one"][1])]
    heads0 = y_swap(v["back0"][1])
    far_h3 = x_swap(v["sum3"][2])
    far_t0 = x_swap(v["sum0"][3])
    there3 = summed([v["sum3"][1], v["far_t3"]])
    two_down = summed(
        [v["sum1"][0], v["far_h1"], v["there1"], v["down2"]], [False, False, True, False]
    )
    there3_got = y_swap(there3)
    two_down_got = z_down(two_down)
    back1 = attn_back(1, after(v["grad_mine"][1], there3, two_down))
    v.update(
        out_two=two, heads0=heads0, far_h3=far_h3, far_t0=far_t0, there3=there3_got, back1=back1
    )
    sync()

    heads1 = y_swap(v["back1"][1])
    far_h0 = x_swap(v["sum0"][2])
    up3 = z_up(summed([v["sum3"][0], v["far_h3"], v["there3"]], turned))
    tables = [v[name] for name in ("cos_part", "sin_part", "gain_q", "gain_k")]
    head0 = head_back(
        info, v["back0"][0], v["heads0"], v["mine"][0][1], v["theirs"][0][1], *tables, heads
    )
    v.update(heads1=heads1, two_down=two_down_got, head0=head0)
    sync()

    there0 = y_swap(summed([v["sum0"][1], v["far_t0"]]))
    head1 = head_back(
        info, v["back1"][0], v["heads1"], v["mine"][1][1], v["theirs"][1][1], *tables, heads
    )
    *tokens_low, gain_one_sum = norm_one_back(
        info,
        [v["head0"][0], head1[0]],
        v["proj_pieces"],
        v["x_in"],
        v["grad_resid"],
        v["gain_one"],
        256,
    )
    v.update(head1=head1, tokens_low=tokens_low, gain_one_sum=gain_one_sum, up3=up3)
    sync()

    tok_one = [z_up(v["tokens_low"][0])]
    tok_three = [z_down(v["tokens_low"][0])]
    grads = []
    for k in range(4):
        grads.append(
            weight_grad(
                after(v["normed_one_t"], *(grads[-1] if grads else ())),
                v[f"head{k % 2}"][0],
                k // 2,
                v["grad_attn_t"],
                v["attended"],
                k,
            )
        )
    came = [core_swap(send) for _, send in grads]
    v.update(tok_one=tok_one, keeps=[keep for keep, _ in grads], came=came, there0=there0)
    v.update(far_h0=far_h0)
    sync()

    tok_one = v["tok_one"] + [z_up(v["tokens_low"][1])]
    sums = []
    for keep, other in zip(v["keeps"], v["came"]):
        sums.append(core_sum(info, after(keep, *(sums[-1] if sums else ())), other))
    far_t = [x_swap(s[3]) for s in sums]
    far_h = [x_swap(s[2]) for s in sums]
    part0 = summed([v["sum0"][0], v["far_h0"], v["there0"]], turned)
    ffn_sum = summed([part0, v["two_down"], v["up3"]], None, F32)
    v.update(tok_three=tok_three, sums=sums, far_t=far_t, ffn_sum=ffn_sum)
    sync()

    tok_three = v["tok_three"] + [z_down(v["tokens_low"][1])]
    there = [y_swap(summed([s[1], far])) for s, far in zip(v["sums"], v["far_t"])]
    v.update(tok_one=tok_one, there=there, far_h=far_h)
    sync()

    parts = [summed([s[0], far, t]) for s, far, t in zip(v["sums"], v["far_h"], v["there"])]
    parts = [parts[0], z_down(parts[1]), z_far(parts[2]), z_up(parts[3])]
    ffn_other = y_swap(v["ffn_sum"])
    tok_two = [z_up(v["tok_one"][0])]
    v.update(parts=parts, tok_three=tok_three, ffn_other=ffn_other)
    sync()

    attn_sum = summed(v["parts"], None, F32)
    attn_other = y_swap(attn_sum)
    tok_two.append(z_up(v["tok_one"][1]))

    def spread(own, one, two, three, dtype):
        out = jnp.zeros((rows_dev, tok, width), dtype)
        for k, parts in ((0, own), (1, one), (3, three), (2, two)):
            row = lax.rem(z - k + 4, 4)
            for j, part in enumerate(parts):
                out = lax.dynamic_update_slice(
                    out, part.astype(dtype)[None], (row, j * tok // 2, 0)
                )
        return out

    tokens_grad = spread(v["tokens_low"], v["tok_one"], tok_two, v["tok_three"], F32)
    output = spread(v["results"], v["one"], v["out_two"], v["out_three"], BF16)

    def finish(own, other):
        return jnp.concatenate(
            [jnp.where(ctx == 0, own, other), jnp.where(ctx == 0, other, own)], axis=0
        )

    ffn_grad = finish(v["ffn_sum"], turn_chunks(v["ffn_other"]))
    attn_grad = finish(attn_sum, attn_other)

    def total(v):
        for axis, pairs in (("fsdp", CORE_SWAP), ("fsdp", X_SWAP), ("ctx", Y_SWAP)):
            v = v + lax.ppermute(v, axis, pairs)
        for pairs in (Z_NEAR, Z_FAR):
            v = v + lax.ppermute(v, "tp", pairs)
        return v

    back = [v["head0"], v["head1"]]
    gain_one_sum, gain_two_sum, square = v["gain_one_sum"], v["gain_two_sum"], v["square"]
    total_count = v["total_count"]
    gain_heads = back[0][1] + back[1][1]
    sums = total(
        jnp.concatenate(
            [
                natural(gain_one_sum.reshape(4, quarter)).reshape(1, width),
                natural(gain_two_sum.reshape(4, quarter)).reshape(1, width),
                gain_heads[:, 0].reshape(1, hd),
                gain_heads[:, 1].reshape(1, hd),
                jnp.sum(square).reshape(1, 1),
                jnp.zeros((1, 127), F32),
            ],
            axis=1,
        )
    )[0]
    teacher_loss = sums[2 * width + 2 * hd] / (total_count * width)

    def own_part(at, size):
        return lax.dynamic_slice_in_dim(sums, at + fsdp * (size // 4), size // 4, 0)

    third = units // 3

    def columns(first):
        starts = [first(j) for j in range(3)]
        parts = [ffn_grad[:, s : s + third] for s in starts]
        return jnp.concatenate(
            [jnp.where(ctx == 0, parts[0], parts[2]), parts[1], jnp.where(ctx == 0, parts[2], parts[0])],
            axis=1,
        )

    return (
        output,
        teacher_loss,
        tokens_grad,
        own_part(0, width),
        attn_grad[:, :q_cols],
        attn_grad[:, q_cols : q_cols + k_cols],
        attn_grad[:, q_cols + k_cols : proj],
        own_part(2 * width, hd),
        own_part(2 * width + hd, hd),
        attn_grad[:, proj:].T,
        own_part(width, width),
        columns(lambda j: 2 * j * third),
        columns(lambda j: (2 * j + 1) * third),
        columns(lambda j: 2 * units + j * third).T,
    )


def solution(mesh):
    return jax.shard_map(
        per_device_rows if fits(mesh) else per_device_any,
        mesh=mesh,
        in_specs=(
            P("fsdp", "ctx", None),
            P("fsdp", "ctx", None),
            P("fsdp"),
            P("fsdp"),
            P("fsdp", "tp"),
            P("fsdp", "tp"),
            P("fsdp", "tp"),
            P("fsdp"),
            P("fsdp"),
            P("tp", "fsdp"),
            P("fsdp"),
            P("fsdp", "tp"),
            P("fsdp", "tp"),
            P("tp", "fsdp"),
        ),
        out_specs=(
            P("fsdp", "ctx", None),
            P(),
            P("fsdp", "ctx", None),
            P("fsdp"),
            P("fsdp", "tp"),
            P("fsdp", "tp"),
            P("fsdp", "tp"),
            P("fsdp"),
            P("fsdp"),
            P("tp", "fsdp"),
            P("fsdp"),
            P("fsdp", "tp"),
            P("fsdp", "tp"),
            P("tp", "fsdp"),
        ),
        check_vma=False,
    )
```

```python
import functools
import math

import jax
import jax.numpy as jnp
from jax import lax
from jax.experimental import pallas as pl
from jax.experimental.pallas import tpu as pltpu
from jax.sharding import PartitionSpec as P

EPS = 1e-05
THETA = 1000000.0
NEGATIVE = -1e30


def rms_scale(field_in, gain_vec):
    return (
        field_in * lax.rsqrt(jnp.mean(field_in * field_in, axis=-1, keepdims=True) + EPS) * gain_vec
    )


def rotate(field_in, positions):
    half_dim = field_in.shape[-1] // 2
    frequency = THETA ** (-(2.0 * jnp.arange(half_dim, dtype=jnp.float32)) / field_in.shape[-1])
    angles = positions[:, None] * frequency[None, :]
    cos_part = jnp.cos(angles)[:, None, :]
    sin_part = jnp.sin(angles)[:, None, :]
    lower_half = field_in[..., :half_dim]
    upper_half = field_in[..., half_dim:]
    return jnp.concatenate(
        [
            lower_half * cos_part - upper_half * sin_part,
            upper_half * cos_part + lower_half * sin_part,
        ],
        axis=-1,
    )


def linear(left_mat, right_mat):
    return jnp.dot(left_mat, right_mat, preferred_element_type=jnp.float32)


def linear_left(left_mat, right_mat):
    return lax.dot_general(
        left_mat, right_mat, (((0,), (0,)), ((), ())), preferred_element_type=jnp.float32
    )


def linear_right(left_mat, right_mat):
    return lax.dot_general(
        left_mat, right_mat, (((1,), (1,)), ((), ())), preferred_element_type=jnp.float32
    )


def swiglu(gate_act, up_act):
    return jax.nn.silu(gate_act) * up_act


def per_device_any(
    tokens,
    teacher,
    lengths,
    attn_gain,
    q_weight,
    k_weight,
    v_weight,
    q_gain,
    k_gain,
    o_weight,
    ffn_gain,
    gate_weight,
    up_weight,
    down_weight,
):
    (
        gain_one,
        w_query,
        w_key,
        w_value,
        gain_query,
        gain_key,
        w_output,
        gain_two,
        w_gate,
        w_upper,
        w_down,
    ) = (
        lax.all_gather(attn_gain, "fsdp", axis=0, tiled=True),
        lax.all_gather(q_weight, "fsdp", axis=0, tiled=True),
        lax.all_gather(k_weight, "fsdp", axis=0, tiled=True),
        lax.all_gather(v_weight, "fsdp", axis=0, tiled=True),
        lax.all_gather(q_gain, "fsdp", axis=0, tiled=True),
        lax.all_gather(k_gain, "fsdp", axis=0, tiled=True),
        lax.all_gather(o_weight, "fsdp", axis=1, tiled=True),
        lax.all_gather(ffn_gain, "fsdp", axis=0, tiled=True),
        lax.all_gather(gate_weight, "fsdp", axis=0, tiled=True),
        lax.all_gather(up_weight, "fsdp", axis=0, tiled=True),
        lax.all_gather(down_weight, "fsdp", axis=1, tiled=True),
    )
    rows_dev, block_len, model_width = tokens.shape
    count_tok = rows_dev * block_len
    head_dim = gain_query.shape[0]
    q_heads = w_query.shape[1] // head_dim
    kv_heads = w_key.shape[1] // head_dim
    group_size = q_heads // kv_heads
    score_scale = head_dim ** (-0.5)
    row_len = block_len * lax.axis_size("ctx")
    key_block = math.gcd(row_len, 512)
    block_start = lax.axis_index("ctx") * block_len
    tiles_used = (block_start + block_len + key_block - 1) // key_block
    slot_pos = block_start + jnp.arange(block_len, dtype=jnp.int32)
    positions = slot_pos.astype(jnp.float32)
    valid = (slot_pos[None, :] < lengths[:, None]).astype(jnp.float32)
    slots = count_tok * lax.axis_size("fsdp") * lax.axis_size("ctx")
    gain_two_f = gain_two.astype(jnp.float32)
    gain_one_f = gain_one.astype(jnp.float32)
    inputs = tokens.astype(jnp.float32)
    normed_one, back_one = jax.vjp(rms_scale, inputs, gain_one_f)
    normed_low = normed_one.astype(jnp.bfloat16).reshape(count_tok, model_width)
    query_raw = linear(normed_low, w_query)
    key_raw = linear(normed_low, w_key)
    value_raw = linear(normed_low, w_value)

    def heads_post(raw_heads, gain_vec):
        shaped = raw_heads.reshape(rows_dev, block_len, -1, head_dim)
        return rotate(rms_scale(shaped, gain_vec), positions)

    query_rot, query_back = jax.vjp(heads_post, query_raw, gain_query.astype(jnp.float32))
    key_rot, key_back = jax.vjp(heads_post, key_raw, gain_key.astype(jnp.float32))
    queries = query_rot.astype(jnp.bfloat16).reshape(
        rows_dev, block_len, kv_heads, group_size, head_dim
    )
    key_rows = key_rot.astype(jnp.bfloat16).reshape(rows_dev, block_len, kv_heads * head_dim)
    values = value_raw.astype(jnp.bfloat16).reshape(rows_dev, block_len, kv_heads * head_dim)
    keys_all, values_all = (
        lax.all_gather(key_rows, "ctx", axis=1, tiled=True),
        lax.all_gather(values, "ctx", axis=1, tiled=True),
    )

    def key_tile(tile_index):
        tile_start = tile_index * key_block
        key_pos = tile_start + jnp.arange(key_block, dtype=jnp.int32)
        key_part = lax.dynamic_slice_in_dim(keys_all, tile_start, key_block, 1).reshape(
            rows_dev, key_block, kv_heads, head_dim
        )
        value_part = lax.dynamic_slice_in_dim(values_all, tile_start, key_block, 1).reshape(
            rows_dev, key_block, kv_heads, head_dim
        )
        scores = (
            jnp.einsum("rqhgd,rkhd->rhgqk", queries, key_part, preferred_element_type=jnp.float32)
            * score_scale
        )
        allowed = (key_pos[None, None, :] <= slot_pos[None, :, None]) & (
            key_pos[None, None, :] < lengths[:, None, None]
        )
        return (tile_start, scores, allowed[:, None, None], key_part, value_part)

    stat_shape = (rows_dev, kv_heads, group_size, block_len)

    def stats_step(tile_index, carried):
        running_max, running_sum = carried
        tile_start, scores, allowed, key_part, value_part = key_tile(tile_index)
        masked = jnp.where(allowed, scores, NEGATIVE)
        new_max = jnp.maximum(running_max, jnp.max(masked, axis=-1))
        terms = jnp.where(allowed, jnp.exp(masked - new_max[..., None]), 0.0)
        return (new_max, running_sum * jnp.exp(running_max - new_max) + jnp.sum(terms, axis=-1))

    running_max, running_sum = lax.fori_loop(
        0,
        tiles_used,
        stats_step,
        (jnp.full(stat_shape, NEGATIVE, jnp.float32), jnp.zeros(stat_shape, jnp.float32)),
    )
    log_total = running_max + jnp.log(running_sum)
    out_shape = (rows_dev, block_len, kv_heads, group_size, head_dim)

    def value_step(tile_index, carried):
        rounded_out, exact_out = carried
        tile_start, scores, allowed, key_part, value_part = key_tile(tile_index)
        tile_probs = jnp.where(allowed, jnp.exp(scores - log_total[..., None]), 0.0)
        rounded_out = rounded_out + jnp.einsum(
            "rhgqk,rkhd->rqhgd",
            tile_probs.astype(jnp.bfloat16),
            value_part,
            preferred_element_type=jnp.float32,
        )
        exact_out = exact_out + jnp.einsum(
            "rhgqk,rkhd->rqhgd", tile_probs, value_part.astype(jnp.float32)
        )
        return (rounded_out, exact_out)

    rounded_out, exact_out = lax.fori_loop(
        0,
        tiles_used,
        value_step,
        (jnp.zeros(out_shape, jnp.float32), jnp.zeros(out_shape, jnp.float32)),
    )
    attended = rounded_out.astype(jnp.bfloat16).reshape(count_tok, q_heads * head_dim)
    attn_total = lax.psum(linear(attended, w_output), "tp")
    resid = inputs + attn_total.reshape(rows_dev, block_len, model_width)
    normed_two, back_two = jax.vjp(rms_scale, resid, gain_two_f)
    normed_second = normed_two.astype(jnp.bfloat16).reshape(count_tok, model_width)
    gate_act = linear(normed_second, w_gate)
    up_act = linear(normed_second, w_upper)
    hidden_full, back_glu = jax.vjp(swiglu, gate_act, up_act)
    hidden = hidden_full.astype(jnp.bfloat16)
    ffn_total = lax.psum(linear(hidden, w_down), "tp")
    result = resid + ffn_total.reshape(rows_dev, block_len, model_width)
    error_value = result - teacher.astype(jnp.float32)
    valid_col = valid[..., None]
    total_square, total_count = lax.psum(
        (jnp.sum(valid_col * error_value * error_value), jnp.sum(valid)), ("fsdp", "ctx")
    )
    teacher_loss = total_square / (total_count * model_width)
    grad_result = valid_col * error_value * (slots / total_count)
    grad_low = grad_result.astype(jnp.bfloat16).reshape(count_tok, model_width)
    grad_down = linear_left(hidden, grad_low)
    grad_hidden = linear_right(grad_low, w_down)
    grad_gate_full, grad_up_full = back_glu(grad_hidden)
    grad_gate = grad_gate_full.astype(jnp.bfloat16)
    grad_up = grad_up_full.astype(jnp.bfloat16)
    grad_wgate = linear_left(normed_second, grad_gate)
    grad_wup = linear_left(normed_second, grad_up)
    normed_two_part = linear_right(grad_gate, w_gate) + linear_right(grad_up, w_upper)
    grad_normed_two = lax.psum(normed_two_part, "tp")
    grad_resid_norm, grad_gain_two = back_two(
        grad_normed_two.reshape(rows_dev, block_len, model_width)
    )
    grad_resid = grad_result + grad_resid_norm
    grad_attn_low = grad_resid.astype(jnp.bfloat16).reshape(count_tok, model_width)
    grad_woutput = linear_left(attended, grad_attn_low)
    grad_attended = linear_right(grad_attn_low, w_output).astype(jnp.bfloat16).reshape(out_shape)
    delta = jnp.einsum("rqhgd,rqhgd->rhgq", grad_attended.astype(jnp.float32), exact_out)
    full_shape = (rows_dev, row_len, kv_heads * head_dim)

    def grad_step(tile_index, carried):
        grad_queries, grad_keys, grad_values = carried
        tile_start, scores, allowed, key_part, value_part = key_tile(tile_index)
        tile_probs = jnp.where(allowed, jnp.exp(scores - log_total[..., None]), 0.0)
        grad_probs = jnp.einsum(
            "rqhgd,rkhd->rhgqk", grad_attended, value_part, preferred_element_type=jnp.float32
        )
        grad_scores = (tile_probs * (grad_probs - delta[..., None])).astype(jnp.bfloat16)
        grad_queries = (
            grad_queries
            + jnp.einsum(
                "rhgqk,rkhd->rqhgd", grad_scores, key_part, preferred_element_type=jnp.float32
            )
            * score_scale
        )
        key_term = (
            jnp.einsum(
                "rhgqk,rqhgd->rkhd", grad_scores, queries, preferred_element_type=jnp.float32
            )
            * score_scale
        )
        value_term = jnp.einsum(
            "rhgqk,rqhgd->rkhd",
            tile_probs.astype(jnp.bfloat16),
            grad_attended,
            preferred_element_type=jnp.float32,
        )
        grad_keys = lax.dynamic_update_slice_in_dim(
            grad_keys, key_term.reshape(rows_dev, key_block, kv_heads * head_dim), tile_start, 1
        )
        grad_values = lax.dynamic_update_slice_in_dim(
            grad_values, value_term.reshape(rows_dev, key_block, kv_heads * head_dim), tile_start, 1
        )
        return (grad_queries, grad_keys, grad_values)

    grad_queries, grad_keys, grad_values = lax.fori_loop(
        0,
        tiles_used,
        grad_step,
        (
            jnp.zeros(out_shape, jnp.float32),
            jnp.zeros(full_shape, jnp.float32),
            jnp.zeros(full_shape, jnp.float32),
        ),
    )
    key_grad, value_grad = (
        lax.psum_scatter(grad_keys, "ctx", scatter_dimension=1, tiled=True),
        lax.psum_scatter(grad_values, "ctx", scatter_dimension=1, tiled=True),
    )
    grad_query_raw, grad_gain_query = query_back(
        grad_queries.reshape(rows_dev, block_len, q_heads, head_dim)
    )
    grad_key_raw, grad_gain_key = key_back(
        key_grad.reshape(rows_dev, block_len, kv_heads, head_dim)
    )
    query_low = grad_query_raw.astype(jnp.bfloat16)
    key_low = grad_key_raw.astype(jnp.bfloat16)
    value_low = value_grad.reshape(count_tok, kv_heads * head_dim).astype(jnp.bfloat16)
    grad_wquery = linear_left(normed_low, query_low)
    grad_wkey = linear_left(normed_low, key_low)
    grad_wvalue = linear_left(normed_low, value_low)
    normed_part = (
        linear_right(query_low, w_query)
        + linear_right(key_low, w_key)
        + linear_right(value_low, w_value)
    )
    grad_normed_one, grad_gain_query, grad_gain_key = lax.psum(
        (normed_part, grad_gain_query, grad_gain_key), "tp"
    )
    grad_input_norm, grad_gain_one = back_one(
        grad_normed_one.reshape(rows_dev, block_len, model_width)
    )
    tokens_grad = grad_resid + grad_input_norm
    partials = (
        grad_gain_one,
        grad_wquery,
        grad_wkey,
        grad_wvalue,
        grad_gain_query,
        grad_gain_key,
        grad_woutput,
        grad_gain_two,
        grad_wgate,
        grad_wup,
        grad_down,
    )
    pieces = (
        lax.psum_scatter(partials[0], ("fsdp", "ctx"), scatter_dimension=0, tiled=True),
        lax.psum_scatter(partials[1], ("fsdp", "ctx"), scatter_dimension=0, tiled=True),
        lax.psum_scatter(partials[2], ("fsdp", "ctx"), scatter_dimension=0, tiled=True),
        lax.psum_scatter(partials[3], ("fsdp", "ctx"), scatter_dimension=0, tiled=True),
        lax.psum_scatter(partials[4], ("fsdp", "ctx"), scatter_dimension=0, tiled=True),
        lax.psum_scatter(partials[5], ("fsdp", "ctx"), scatter_dimension=0, tiled=True),
        lax.psum_scatter(partials[6], ("fsdp", "ctx"), scatter_dimension=1, tiled=True),
        lax.psum_scatter(partials[7], ("fsdp", "ctx"), scatter_dimension=0, tiled=True),
        lax.psum_scatter(partials[8], ("fsdp", "ctx"), scatter_dimension=0, tiled=True),
        lax.psum_scatter(partials[9], ("fsdp", "ctx"), scatter_dimension=0, tiled=True),
        lax.psum_scatter(partials[10], ("fsdp", "ctx"), scatter_dimension=1, tiled=True),
    )
    summed = (
        lax.all_gather(pieces[0], "ctx", axis=0, tiled=True),
        lax.all_gather(pieces[1], "ctx", axis=0, tiled=True),
        lax.all_gather(pieces[2], "ctx", axis=0, tiled=True),
        lax.all_gather(pieces[3], "ctx", axis=0, tiled=True),
        lax.all_gather(pieces[4], "ctx", axis=0, tiled=True),
        lax.all_gather(pieces[5], "ctx", axis=0, tiled=True),
        lax.all_gather(pieces[6], "ctx", axis=1, tiled=True),
        lax.all_gather(pieces[7], "ctx", axis=0, tiled=True),
        lax.all_gather(pieces[8], "ctx", axis=0, tiled=True),
        lax.all_gather(pieces[9], "ctx", axis=0, tiled=True),
        lax.all_gather(pieces[10], "ctx", axis=1, tiled=True),
    )
    return (
        result.astype(jnp.bfloat16),
        teacher_loss,
        tokens_grad,
        summed[0],
        summed[1],
        summed[2],
        summed[3],
        summed[4],
        summed[5],
        summed[6],
        summed[7],
        summed[8],
        summed[9],
        summed[10],
    )


BF16 = jnp.bfloat16
F32 = jnp.float32
LOG2E = math.log2(math.e)
X_SWAP = [(0, 2), (2, 0), (1, 3), (3, 1)]
CORE_SWAP = [(0, 1), (1, 0), (2, 3), (3, 2)]
Y_SWAP = [(0, 1), (1, 0)]
Z_UP = [(0, 1), (1, 2), (2, 3), (3, 0)]
Z_DOWN = [(0, 3), (1, 0), (2, 1), (3, 2)]
Z_NEAR = [(0, 1), (1, 0), (2, 3), (3, 2)]
Z_FAR = [(0, 2), (2, 0), (1, 3), (3, 1)]
MASKS = (0, 2, 1, 3)
ANY = pl.BlockSpec(memory_space=pl.ANY)
SMEM = pl.BlockSpec(memory_space=pltpu.SMEM)


def fits(mesh):
    return dict(mesh.shape) == {"fsdp": 4, "ctx": 2, "tp": 4}


def dot(left, right, left_dim, right_dim):
    return lax.dot_general(
        left, right, (((left_dim,), (right_dim,)), ((), ())), preferred_element_type=F32
    )


def sigmoid(v):
    return 0.5 * jnp.tanh(0.5 * v) + 0.5


def whole(shape):
    zeros = (0,) * len(shape)
    return pl.BlockSpec(shape, lambda *_: zeros, pipeline_mode=pl.Buffered(1))


def settings(dims, mib):
    return pltpu.CompilerParams(
        dimension_semantics=("arbitrary",) * dims, vmem_limit_bytes=mib << 20
    )


def shape_of(shape, dtype):
    return jax.ShapeDtypeStruct(shape, dtype)


def cost(large):
    size = 1 << 42 if large else 1 << 10
    return pl.CostEstimate(flops=size, bytes_accessed=size >> 12, transcendentals=0)


def pack_kernel(info, o_in, g_in, u_in, d_in, out_ref, ffn_ref, o_ref, g_ref, u_ref, d_ref, sems):
    ctx = info[2]
    pairs = ((o_in, o_ref), (g_in, g_ref), (u_in, u_ref), (d_in, d_ref))
    copies = [pltpu.make_async_copy(a, b, sems.at[i]) for i, (a, b) in enumerate(pairs)]
    for copy in copies:
        copy.start()
    for copy in copies:
        copy.wait()
    out_ref[...] = o_ref[...].astype(F32).T.astype(BF16)
    third = g_ref.shape[1] // 3
    for j in range(3):
        at = pl.multiple_of(jnp.where(ctx == 0, j, 2 - j) * third, third)
        base = 3 * third * j
        ffn_ref[:, base : base + third] = g_ref[:, pl.ds(at, third)]
        ffn_ref[:, base + third : base + 2 * third] = u_ref[:, pl.ds(at, third)]
        down = d_ref[pl.ds(at, third), :].astype(F32).T.astype(BF16)
        ffn_ref[:, base + 2 * third : base + 3 * third] = down


def pack(info, o, g, u, d):
    rows = g.shape[0]
    return pl.pallas_call(
        pack_kernel,
        in_specs=[SMEM] + [ANY] * 4,
        out_specs=[pl.BlockSpec(memory_space=pltpu.VMEM)] * 2,
        out_shape=[shape_of((rows, o.shape[0]), BF16), shape_of((rows, 3 * g.shape[1]), BF16)],
        scratch_shapes=[pltpu.VMEM(a.shape, BF16) for a in (o, g, u, d)]
        + [pltpu.SemaphoreType.DMA((4,))],
        compiler_params=pltpu.CompilerParams(vmem_limit_bytes=24 << 20),
        cost_estimate=cost(False),
        name="pack",
    )(info, o, g, u, d)


def join_kernel(q_ref, k_ref, v_ref, out_ref):
    at = 0
    for ref in (q_ref, k_ref, v_ref):
        out_ref[:, at : at + ref.shape[1]] = ref[...]
        at += ref.shape[1]


def join(q, k, v):
    return pl.pallas_call(
        join_kernel,
        out_shape=shape_of((q.shape[0], q.shape[1] + k.shape[1] + v.shape[1]), BF16),
        compiler_params=pltpu.CompilerParams(vmem_limit_bytes=8 << 20),
        cost_estimate=cost(False),
        name="join",
    )(q, k, v)


def norm_one_kernel(info, tok_ref, gain_ref, x_ref, nt_ref, x32):
    quarter = x_ref.shape[1] // 4
    for p, mask in enumerate(MASKS):
        at = pl.multiple_of(jnp.bitwise_xor(info[1], mask) * quarter, quarter)
        part = tok_ref[0, :, pl.ds(at, quarter)]
        x_ref[:, p * quarter : (p + 1) * quarter] = part
        x32[:, p * quarter : (p + 1) * quarter] = part.astype(F32)
    x = x32[...]
    rho = lax.rsqrt(jnp.mean(x * x, axis=-1, keepdims=True) + EPS)
    nt_ref[...] = (x * rho * gain_ref[...]).T.astype(BF16)


def norm_one(info, tokens, gain, tile):
    _, tok, width = tokens.shape
    return pl.pallas_call(
        norm_one_kernel,
        grid_spec=pltpu.PrefetchScalarGridSpec(
            num_scalar_prefetch=1,
            grid=(tok // tile,),
            in_specs=[
                pl.BlockSpec((1, tile, width), lambda i, info: (info[0], i, 0)),
                pl.BlockSpec((1, width), lambda i, info: (0, 0)),
            ],
            out_specs=[
                pl.BlockSpec((tile, width), lambda i, info: (i, 0)),
                pl.BlockSpec((width, tile), lambda i, info: (0, i)),
            ],
            scratch_shapes=[pltpu.VMEM((tile, width), F32)],
        ),
        out_shape=[shape_of((tok, width), BF16), shape_of((width, tok), BF16)],
        compiler_params=settings(1, 24),
        cost_estimate=cost(False),
        name="norm_one",
    )(info, tokens, gain)


def proj_kernel(heads, block, plan, count, info, *refs):
    nt_ref, cos_ref, sin_ref, qg_ref, kg_ref, rot_ref, raw_ref, w_ref, sem = refs[count:]
    rows = w_ref.shape[0] // 4

    @pl.when(pl.program_id(0) == 0)
    def _():
        for k in range(4):

            @pl.when(block(info) == k)
            def _():
                for p, (piece, row) in enumerate(plan[k]):
                    src = refs[piece].at[pl.ds(row, rows)]
                    pltpu.make_async_copy(src, w_ref.at[pl.ds(p * rows, rows)], sem).start()

        pltpu.make_async_copy(w_ref, w_ref, sem).wait()

    hd = qg_ref.shape[0]
    half = hd // 2
    raw = dot(w_ref[...], nt_ref[...], 0, 0)
    cos_part, sin_part = cos_ref[...], sin_ref[...]
    heads_q, heads_k = heads
    raw_ref[...] = raw.astype(BF16)
    for h in range(heads_q + heads_k):
        v = raw[h * hd : (h + 1) * hd]
        rho = lax.rsqrt(jnp.mean(v * v, axis=0, keepdims=True) + EPS)
        v = v * rho * (qg_ref[...] if h < heads_q else kg_ref[...])
        a, b = v[:half], v[half:]
        rot_ref[h * hd : h * hd + half, :] = (a * cos_part - b * sin_part).astype(BF16)
        rot_ref[h * hd + half : (h + 1) * hd, :] = (b * cos_part + a * sin_part).astype(BF16)
    at = (heads_q + heads_k) * hd
    rot_ref[at:, :] = raw[at:].astype(BF16)


def project(info, weights, normed_t, cos_part, sin_part, gain_q, gain_k, heads, block):
    plan, pieces = weights
    width, tok = normed_t.shape
    cols = pieces[0].shape[1]
    tile = min(512, tok)
    const = lambda a: pl.BlockSpec(a.shape, lambda i, info: (0, 0))
    tab = lambda a: pl.BlockSpec((a.shape[0], tile), lambda i, info: (0, i))
    return pl.pallas_call(
        functools.partial(proj_kernel, heads, block, plan, len(pieces)),
        grid_spec=pltpu.PrefetchScalarGridSpec(
            num_scalar_prefetch=1,
            grid=(tok // tile,),
            in_specs=[ANY] * len(pieces)
            + [tab(normed_t), tab(cos_part), tab(sin_part), const(gain_q), const(gain_k)],
            out_specs=[pl.BlockSpec((cols, tile), lambda i, info: (0, i))] * 2,
            scratch_shapes=[pltpu.VMEM((width, cols), BF16), pltpu.SemaphoreType.DMA],
        ),
        out_shape=[shape_of((cols, tok), BF16), shape_of((cols, tok), BF16)],
        compiler_params=settings(1, 24),
        cost_estimate=cost(False),
        name="project",
    )(info, *pieces, normed_t, cos_part, sin_part, gain_q, gain_k)


def head_back_kernel(
    heads, info, dm_ref, dt_ref, rm_ref, rt_ref, cos_ref, sin_ref, qg_ref, kg_ref, out_ref, gg_ref
):
    step, part = pl.program_id(0), pl.program_id(1)
    hd = qg_ref.shape[0]
    half = hd // 2
    heads_q, heads_k = heads
    cos_part, sin_part = cos_ref[...], sin_ref[...]
    tile = cos_part.shape[1]

    @pl.when((step == 0) & (part == 0))
    def _():
        gg_ref[...] = jnp.zeros_like(gg_ref)

    def work(d_ref, r_ref):
        gain_q = jnp.zeros((hd, 1), F32)
        gain_k = jnp.zeros((hd, 1), F32)
        done = []
        for h in range(heads_q + heads_k):
            is_q = h < heads_q
            g = d_ref[h * hd : (h + 1) * hd, :].astype(F32)
            raw = r_ref[h * hd : (h + 1) * hd, :].astype(F32)
            a, b = g[:half], g[half:]
            turned = jnp.concatenate(
                [a * cos_part + b * sin_part, b * cos_part - a * sin_part], axis=0
            )
            rho = lax.rsqrt(jnp.mean(raw * raw, axis=0, keepdims=True) + EPS)
            unit = raw * rho
            prod = turned * unit
            scaled = turned * (qg_ref[...] if is_q else kg_ref[...])
            mean = jnp.mean(scaled * unit, axis=0, keepdims=True)
            done.append(rho * (scaled - unit * mean))
            total = jnp.sum(prod, axis=1, keepdims=True)
            if is_q:
                gain_q = gain_q + total
            else:
                gain_k = gain_k + total
        done.append(d_ref[(heads_q + heads_k) * hd :, :].astype(F32))
        out_ref[0] = jnp.concatenate(done, axis=0).T.astype(BF16)
        lane = lax.broadcasted_iota(jnp.int32, gg_ref.shape, 1)
        gg_ref[...] += jnp.where(lane == 0, gain_q, jnp.where(lane == 1, gain_k, 0.0))

    @pl.when(step == 0)
    def _():
        work(dm_ref, rm_ref)

    @pl.when(step == 1)
    def _():
        work(dt_ref, rt_ref)


def head_back(info, grad_mine, grad_theirs, raw_mine, raw_theirs, cos_part, sin_part, gq, gk, heads):
    cols, tok = grad_mine.shape
    tile = min(512, tok)
    mine = pl.BlockSpec((cols, tile), lambda s, i, info: (0, jnp.where(s == 0, i, tok // tile - 1)))
    theirs = pl.BlockSpec((cols, tile), lambda s, i, info: (0, jnp.where(s == 0, 0, i)))
    tab = lambda a: pl.BlockSpec((a.shape[0], tile), lambda s, i, info: (0, i))
    const = lambda a: pl.BlockSpec(a.shape, lambda s, i, info: (0, 0))
    return pl.pallas_call(
        functools.partial(head_back_kernel, heads),
        grid_spec=pltpu.PrefetchScalarGridSpec(
            num_scalar_prefetch=1,
            grid=(2, tok // tile),
            in_specs=[
                mine,
                theirs,
                mine,
                theirs,
                tab(cos_part),
                tab(sin_part),
                const(gq),
                const(gk),
            ],
            out_specs=[
                pl.BlockSpec(
                    (1, tile, cols), lambda s, i, info: (jnp.bitwise_xor(info[2], s), i, 0)
                ),
                pl.BlockSpec((gq.shape[0], 128), lambda s, i, info: (0, 0)),
            ],
        ),
        out_shape=[shape_of((2, tok, cols), BF16), shape_of((gq.shape[0], 128), F32)],
        compiler_params=settings(2, 24),
        cost_estimate=cost(False),
        name="head_back",
    )(info, grad_mine, grad_theirs, raw_mine, raw_theirs, cos_part, sin_part, gq, gk)


def load_rows(info, mine_ref, got_ref, rows, sems):
    tok = mine_ref.shape[1]
    ctx = info[2]
    here = pl.multiple_of(ctx * tok, tok)
    there = pl.multiple_of((1 - ctx) * tok, tok)
    one = pltpu.make_async_copy(mine_ref, rows.at[:, pl.ds(here, tok)], sems.at[0])
    two = pltpu.make_async_copy(got_ref, rows.at[:, pl.ds(there, tok)], sems.at[1])
    one.start()
    two.start()
    one.wait()
    two.wait()


def keys_with_bias(keys, length):
    hd, slots = keys.shape
    pos = lax.broadcasted_iota(jnp.int32, (hd, slots), 1)
    row = lax.broadcasted_iota(jnp.int32, (hd, slots), 0)
    bias = jnp.where((row == 0) & (pos >= length), NEGATIVE, 0.0)
    return jnp.concatenate([keys.astype(F32), bias], axis=0).T.astype(BF16)


def query_with_one(pair):
    one_row = jnp.where(lax.broadcasted_iota(jnp.int32, pair.shape, 0) == 0, 1.0, 0.0)
    return jnp.concatenate([pair, one_row.astype(BF16)], axis=0)


def causal(scores, width):
    key_pos = lax.broadcasted_iota(jnp.int32, (width, width), 0)
    query_pos = lax.broadcasted_iota(jnp.int32, (width, width), 1)
    allowed = key_pos <= query_pos
    return jnp.where(jnp.concatenate([allowed, allowed], axis=1), scores, NEGATIVE)


def attn_fwd_kernel(
    width, hd, info, mine_ref, got_ref, keep_ref, send_ref, lse_ref, rows, key_rows, sems
):
    head, block = pl.program_id(0), pl.program_id(1)
    heads_k = pl.num_programs(0)
    scale = hd**-0.5 * LOG2E
    length = info[3]
    key_at = pl.multiple_of(heads_k * 2 * hd + head * hd, hd)
    value_at = pl.multiple_of(heads_k * 3 * hd + head * hd, hd)
    query_at = pl.multiple_of(head * 2 * hd, 2 * hd)

    @pl.when((head == 0) & (block == 0))
    def _():
        load_rows(info, mine_ref, got_ref, rows, sems)

    @pl.when(block == 0)
    def _():
        key_rows[...] = keys_with_bias(rows[pl.ds(key_at, hd), :], length)

    start = pl.multiple_of(block * width, width)
    both = rows[pl.ds(query_at, 2 * hd), pl.ds(start, width)]
    query = query_with_one(jnp.concatenate([both[:hd], both[hd:]], axis=1))

    def tile(at, carried, diagonal):
        out, total = carried
        scores = dot(key_rows[pl.ds(at, width), :], query, 1, 0)
        if diagonal:
            scores = causal(scores, width)
        probs = jnp.exp2(scores * scale)
        total = total + jnp.sum(probs, axis=0, keepdims=True)
        out = out + dot(rows[pl.ds(value_at, hd), pl.ds(at, width)], probs.astype(BF16), 1, 0)
        return out, total

    carried = (jnp.zeros((hd, 2 * width), F32), jnp.zeros((1, 2 * width), F32))
    full = jnp.minimum(block, lax.div(length + width - 1, width))
    carried = lax.fori_loop(
        0, full, lambda j, c: tile(pl.multiple_of(j * width, width), c, False), carried
    )
    out, total = tile(start, carried, True)
    out = out * (1.0 / total)
    out = jnp.concatenate([out[:, :width], out[:, width:]], axis=0).T.astype(BF16)
    here = block // 2 == info[2]

    @pl.when(here)
    def _():
        keep_ref[...] = out

    @pl.when(jnp.logical_not(here))
    def _():
        send_ref[...] = out

    log_total = jnp.log2(total)
    lse_ref[0, 0:1, :] = log_total[:, :width]
    lse_ref[0, 1:2, :] = log_total[:, width:]


def keep_block(i, info):
    return jnp.clip(i - 2 * info[2], 0, 1)


def send_block(i, info):
    return jnp.clip(i - 2 * (1 - info[2]), 0, 1)


def attn_fwd(info, mine, got, hd):
    cols, tok = mine.shape
    heads_k = cols // (4 * hd)
    width = tok // 2
    return pl.pallas_call(
        functools.partial(attn_fwd_kernel, width, hd),
        grid_spec=pltpu.PrefetchScalarGridSpec(
            num_scalar_prefetch=1,
            grid=(heads_k, 4),
            in_specs=[ANY, ANY],
            out_specs=[
                pl.BlockSpec((width, 2 * hd), lambda h, i, info: (keep_block(i, info), h)),
                pl.BlockSpec((width, 2 * hd), lambda h, i, info: (send_block(i, info), h)),
                pl.BlockSpec((1, 2, width), lambda h, i, info: (h, 0, i)),
            ],
            scratch_shapes=[
                pltpu.VMEM((cols, 2 * tok), BF16),
                pltpu.VMEM((2 * tok, 2 * hd), BF16),
                pltpu.SemaphoreType.DMA((2,)),
            ],
        ),
        out_shape=[
            shape_of((tok, heads_k * 2 * hd), BF16),
            shape_of((tok, heads_k * 2 * hd), BF16),
            shape_of((heads_k, 2, 2 * tok), F32),
        ],
        compiler_params=settings(2, 60),
        cost_estimate=cost(True),
        name="attn_fwd",
    )(info, mine, got)


def attn_bwd_kernel(
    width,
    hd,
    info,
    mine_ref,
    got_ref,
    ok_ref,
    os_ref,
    gk_ref,
    gs_ref,
    lse_ref,
    keep_ref,
    send_ref,
    rows,
    key_rows,
    value_rows,
    key_sum,
    value_sum,
    sems,
):
    head, block = pl.program_id(0), pl.program_id(1)
    heads_k = pl.num_programs(0)
    scale = hd**-0.5
    length = info[3]
    ctx = info[2]
    tok = keep_ref.shape[1]
    key_at = pl.multiple_of(heads_k * 2 * hd + head * hd, hd)
    value_at = pl.multiple_of(heads_k * 3 * hd + head * hd, hd)
    query_at = pl.multiple_of(head * 2 * hd, 2 * hd)

    @pl.when((head == 0) & (block == 0))
    def _():
        load_rows(info, mine_ref, got_ref, rows, sems)

    @pl.when(block == 0)
    def _():
        key_rows[...] = keys_with_bias(rows[pl.ds(key_at, hd), :], length)
        value_rows[...] = rows[pl.ds(value_at, hd), :].astype(F32).T.astype(BF16)
        key_sum[...] = jnp.zeros_like(key_sum)
        value_sum[...] = jnp.zeros_like(value_sum)

    start = pl.multiple_of(block * width, width)
    here = block // 2 == ctx

    def store_query(value):
        at = pl.ds(pl.multiple_of((block % 2) * width, width), width)

        @pl.when(here)
        def _():
            keep_ref[pl.ds(query_at, 2 * hd), at] = value

        @pl.when(jnp.logical_not(here))
        def _():
            send_ref[pl.ds(query_at, 2 * hd), at] = value

    @pl.when(block * width < length)
    def _():
        both = rows[pl.ds(query_at, 2 * hd), pl.ds(start, width)]
        pair = jnp.concatenate([both[:hd], both[hd:]], axis=1)
        query = query_with_one(pair)
        query_rows = pair.astype(F32).T.astype(BF16)
        grad_wide = jnp.where(here, gk_ref[...].astype(F32), gs_ref[...].astype(F32))
        out_wide = jnp.where(here, ok_ref[...].astype(F32), os_ref[...].astype(F32))
        grad_rows = jnp.concatenate([grad_wide[:, :hd], grad_wide[:, hd:]], axis=0).astype(BF16)
        grad_t = grad_wide.T
        prod = (grad_wide * out_wide).T
        grad = jnp.concatenate([grad_t[:hd], grad_t[hd:]], axis=1).astype(BF16)
        delta = jnp.concatenate(
            [
                jnp.sum(prod[:hd], axis=0, keepdims=True),
                jnp.sum(prod[hd:], axis=0, keepdims=True),
            ],
            axis=1,
        )
        lse = jnp.concatenate([lse_ref[0, 0:1, :], lse_ref[0, 1:2, :]], axis=1)

        def tile(at, query_sum, diagonal):
            scores = dot(key_rows[pl.ds(at, width), :], query, 1, 0)
            if diagonal:
                scores = causal(scores, width)
            probs = jnp.exp2(scores * (scale * LOG2E) - lse)
            grad_probs = dot(value_rows[pl.ds(at, width), :], grad, 1, 0)
            grad_scores = (probs * (grad_probs - delta)).astype(BF16)
            value_sum[pl.ds(at, width), :] += dot(probs.astype(BF16), grad_rows, 1, 0)
            key_sum[pl.ds(at, width), :] += dot(grad_scores, query_rows, 1, 0)
            return query_sum + dot(rows[pl.ds(key_at, hd), pl.ds(at, width)], grad_scores, 1, 0)

        query_sum = lax.fori_loop(
            0,
            block,
            lambda j, s: tile(pl.multiple_of(j * width, width), s, False),
            jnp.zeros((hd, 2 * width), F32),
        )
        query_sum = tile(start, query_sum, True) * scale
        store_query(
            jnp.concatenate([query_sum[:, :width], query_sum[:, width:]], axis=0).astype(BF16)
        )

    @pl.when(block * width >= length)
    def _():
        store_query(jnp.zeros((2 * hd, width), BF16))

    @pl.when(block == 3)
    def _():
        for at, total in ((key_at, key_sum[...] * scale), (value_at, value_sum[...])):
            total = total.T.astype(BF16)
            left, right = total[:, :tok], total[:, tok:]

            @pl.when(ctx == 0)
            def _():
                keep_ref[pl.ds(at, hd), :] = left
                send_ref[pl.ds(at, hd), :] = right

            @pl.when(ctx == 1)
            def _():
                keep_ref[pl.ds(at, hd), :] = right
                send_ref[pl.ds(at, hd), :] = left


def attn_bwd(info, mine, got, out_keep, out_send, grad_keep, grad_send, lse, hd):
    cols, tok = mine.shape
    heads_k = cols // (4 * hd)
    width = tok // 2
    keep = pl.BlockSpec((width, 2 * hd), lambda h, i, info: (keep_block(i, info), h))
    send = pl.BlockSpec((width, 2 * hd), lambda h, i, info: (send_block(i, info), h))
    full = pl.BlockSpec((cols, tok), lambda h, i, info: (0, 0))
    return pl.pallas_call(
        functools.partial(attn_bwd_kernel, width, hd),
        grid_spec=pltpu.PrefetchScalarGridSpec(
            num_scalar_prefetch=1,
            grid=(heads_k, 4),
            in_specs=[
                ANY,
                ANY,
                keep,
                send,
                keep,
                send,
                pl.BlockSpec((1, 2, width), lambda h, i, info: (h, 0, i)),
            ],
            out_specs=[full, full],
            scratch_shapes=[
                pltpu.VMEM((cols, 2 * tok), BF16),
                pltpu.VMEM((2 * tok, 2 * hd), BF16),
                pltpu.VMEM((2 * tok, hd), BF16),
                pltpu.VMEM((2 * tok, hd), F32),
                pltpu.VMEM((2 * tok, hd), F32),
                pltpu.SemaphoreType.DMA((2,)),
            ],
        ),
        out_shape=[shape_of((cols, tok), BF16), shape_of((cols, tok), BF16)],
        compiler_params=settings(2, 60),
        cost_estimate=cost(True),
        name="attn_bwd",
    )(info, mine, got, out_keep, out_send, grad_keep, grad_send, lse)


def load_blocks(plan, pieces, target, sem):
    rows = target.shape[1] // 4

    @pl.when(pl.program_id(0) == 0)
    def _():
        for k, places in enumerate(plan):
            for p, (piece, row) in enumerate(places):
                src = pieces[piece].at[pl.ds(row, rows)]
                pltpu.make_async_copy(src, target.at[k, pl.ds(p * rows, rows)], sem).start()
        pltpu.make_async_copy(target, target, sem).wait()


def out_proj_kernel(plan, count, info, *refs):
    x_ref, a0, a1, b0, b1, gain_ref, r_ref, n_ref, nt_ref, att_ref, w_ref, sem = refs[count:]
    load_blocks(plan, refs, w_ref, sem)
    ctx = info[2]
    total = x_ref[...].astype(F32)
    for j, ref, side in ((0, a0, ctx), (1, a1, ctx), (0, b0, 1 - ctx), (1, b1, 1 - ctx)):
        block = 2 * side + j
        part = ref[...]
        att_ref[block] = part
        total = total + dot(part, w_ref[block], 1, 1)
    rho = lax.rsqrt(jnp.mean(total * total, axis=-1, keepdims=True) + EPS)
    normed = total * rho * gain_ref[...]
    r_ref[...] = total
    n_ref[...] = normed.astype(BF16)
    nt_ref[...] = normed.T.astype(BF16)


def out_proj(info, x, mine, theirs, weights, gain, tile):
    plan, pieces = weights
    tok, width = x.shape
    feats = pieces[0].shape[1]
    rows_of = lambda n: pl.BlockSpec((tile, n), lambda i, info: (i, 0))
    return pl.pallas_call(
        functools.partial(out_proj_kernel, plan, len(pieces)),
        grid_spec=pltpu.PrefetchScalarGridSpec(
            num_scalar_prefetch=1,
            grid=(tok // tile,),
            in_specs=[ANY] * len(pieces)
            + [rows_of(width)]
            + [rows_of(feats)] * 4
            + [pl.BlockSpec((1, width), lambda i, info: (0, 0))],
            out_specs=[
                rows_of(width),
                rows_of(width),
                pl.BlockSpec((width, tile), lambda i, info: (0, i)),
                pl.BlockSpec((4, tile, feats), lambda i, info: (0, i, 0)),
            ],
            scratch_shapes=[pltpu.VMEM((4, width, feats), BF16), pltpu.SemaphoreType.DMA],
        ),
        out_shape=[
            shape_of((tok, width), F32),
            shape_of((tok, width), BF16),
            shape_of((width, tok), BF16),
            shape_of((4, tok, feats), BF16),
        ],
        compiler_params=settings(1, 32),
        cost_estimate=cost(True),
        name="out_proj",
    )(info, *pieces, x, *mine, *theirs, gain)


def norm_two_back_kernel(plan, count, info, *refs):
    g_ref, r_ref, gr_ref, gain_ref, gres_ref, gat_ref, a0, a1, b0, b1, gg_ref, w_ref, sem = refs[count:]
    load_blocks(plan, refs, w_ref, sem)
    ctx = info[2]
    grad, resid = g_ref[...], r_ref[...]
    rho = lax.rsqrt(jnp.mean(resid * resid, axis=-1, keepdims=True) + EPS)
    unit = resid * rho
    scaled = grad * gain_ref[...]
    back = rho * (scaled - unit * jnp.mean(scaled * unit, axis=-1, keepdims=True))
    total = gr_ref[...] + back
    gres_ref[...] = total
    low = total.astype(BF16)
    gat_ref[...] = total.T.astype(BF16)

    @pl.when(pl.program_id(0) == 0)
    def _():
        gg_ref[...] = jnp.zeros_like(gg_ref)

    gg_ref[...] += jnp.sum(grad * unit, axis=0, keepdims=True)
    for j, ref, side in ((0, a0, ctx), (1, a1, ctx), (0, b0, 1 - ctx), (1, b1, 1 - ctx)):
        ref[...] = dot(low, w_ref[2 * side + j], 1, 0).astype(BF16)


def norm_two_back(info, grad, resid, grad_result, gain, weights, tile):
    plan, pieces = weights
    tok, width = grad.shape
    feats = pieces[0].shape[1]
    rows_of = lambda n: pl.BlockSpec((tile, n), lambda i, info: (i, 0))
    row = pl.BlockSpec((1, width), lambda i, info: (0, 0))
    return pl.pallas_call(
        functools.partial(norm_two_back_kernel, plan, len(pieces)),
        grid_spec=pltpu.PrefetchScalarGridSpec(
            num_scalar_prefetch=1,
            grid=(tok // tile,),
            in_specs=[ANY] * len(pieces) + [rows_of(width)] * 3 + [row],
            out_specs=[rows_of(width), pl.BlockSpec((width, tile), lambda i, info: (0, i))]
            + [rows_of(feats)] * 4
            + [row],
            scratch_shapes=[pltpu.VMEM((4, width, feats), BF16), pltpu.SemaphoreType.DMA],
        ),
        out_shape=[shape_of((tok, width), F32), shape_of((width, tok), BF16)]
        + [shape_of((tok, feats), BF16)] * 4
        + [shape_of((1, width), F32)],
        compiler_params=settings(1, 32),
        cost_estimate=cost(True),
        name="norm_two_back",
    )(info, *pieces, grad, resid, grad_result, gain)


def norm_one_back_kernel(plan, count, info, *refs):
    p0, p1, x_ref, gres_ref, gain_ref, outa_ref, outb_ref, gg_ref, w_ref, sem = refs[count:]
    load_blocks(plan, refs, w_ref, sem)
    quarter = x_ref.shape[1] // 4
    grad = dot(p0[0], w_ref[0], 1, 1)
    grad = grad + dot(p1[0], w_ref[1], 1, 1)
    grad = grad + dot(p0[1], w_ref[2], 1, 1)
    grad = grad + dot(p1[1], w_ref[3], 1, 1)
    x = x_ref[...].astype(F32)
    rho = lax.rsqrt(jnp.mean(x * x, axis=-1, keepdims=True) + EPS)
    unit = x * rho
    scaled = grad * gain_ref[...]
    back = rho * (scaled - unit * jnp.mean(scaled * unit, axis=-1, keepdims=True))
    total = (gres_ref[...] + back).astype(BF16)
    for p, mask in enumerate(MASKS):
        at = pl.multiple_of(jnp.bitwise_xor(info[1], mask) * quarter, quarter)
        part = total[:, p * quarter : (p + 1) * quarter]

        @pl.when(pl.program_id(0) < pl.num_programs(0) // 2)
        def _():
            outa_ref[:, pl.ds(at, quarter)] = part

        @pl.when(pl.program_id(0) >= pl.num_programs(0) // 2)
        def _():
            outb_ref[:, pl.ds(at, quarter)] = part

    @pl.when(pl.program_id(0) == 0)
    def _():
        gg_ref[...] = jnp.zeros_like(gg_ref)

    gg_ref[...] += jnp.sum(grad * unit, axis=0, keepdims=True)


def norm_one_back(info, pairs, weights, x, grad_resid, gain, tile):
    plan, pieces = weights
    tok, width = x.shape
    cols = pieces[0].shape[1]
    rows_of = lambda n: pl.BlockSpec((tile, n), lambda i, info: (i, 0))
    pair = pl.BlockSpec((2, tile, cols), lambda i, info: (0, i, 0))
    half = tok // tile // 2
    row = pl.BlockSpec((1, width), lambda i, info: (0, 0))
    return pl.pallas_call(
        functools.partial(norm_one_back_kernel, plan, len(pieces)),
        grid_spec=pltpu.PrefetchScalarGridSpec(
            num_scalar_prefetch=1,
            grid=(tok // tile,),
            in_specs=[ANY] * len(pieces) + [pair, pair, rows_of(width), rows_of(width), row],
            out_specs=[
                pl.BlockSpec((tile, width), lambda i, info: (jnp.minimum(i, half - 1), 0)),
                pl.BlockSpec((tile, width), lambda i, info: (jnp.maximum(i - half, 0), 0)),
                row,
            ],
            scratch_shapes=[pltpu.VMEM((4, width, cols), BF16), pltpu.SemaphoreType.DMA],
        ),
        out_shape=[shape_of((tok // 2, width), BF16)] * 2 + [shape_of((1, width), F32)],
        compiler_params=settings(1, 32),
        cost_estimate=cost(True),
        name="norm_one_back",
    )(info, *pieces, *pairs, x, grad_resid, gain)


def weight_copies(plan, pieces, gate_up, down, gate_up_sem, down_sem):
    third = down.shape[1] // 3
    rows = down.shape[0] // 4
    wide, thin = [], []
    for p, chunks in enumerate(plan):
        block = pl.ds(p * rows, rows)
        for j, (piece, row, at) in enumerate(chunks):
            src = pieces[piece].at[pl.ds(row, rows)]
            wide.append(
                pltpu.make_async_copy(
                    src.at[:, pl.ds(at, 2 * third)],
                    gate_up.at[block, pl.ds(j * 2 * third, 2 * third)],
                    gate_up_sem,
                )
            )
            thin.append(
                pltpu.make_async_copy(
                    src.at[:, pl.ds(at + 2 * third, third)],
                    down.at[block, pl.ds(j * third, third)],
                    down_sem,
                )
            )
    return wide, thin


def split_act(act):
    third = act.shape[1] // 6
    part = lambda j: act[:, j * third : (j + 1) * third]
    return [(part(0), part(1)), (part(2), part(3)), (part(4), part(5))]


def ffn_fwd_kernel(tile, plans, last, info, scale, x_ref, in_ref, *rest):
    if last:
        teach_ref, rest = rest[0], rest[1:]
    pieces = []
    for plan in plans:
        count = 1 + max(place[0] for chunks in plan for place in chunks)
        pieces.append(rest[:count])
        rest = rest[count:]
    act_ref, hid_ref = rest[:2]
    if last:
        outa_ref, outb_ref, gres_ref, low_ref, lowt_ref, sq_ref = rest[2:8]
        gate_up, down, total, sems = rest[8:]
    else:
        sum_ref, gate_up, down, total, sems = rest[2:]
    step, part = pl.program_id(0), pl.program_id(1)
    final = len(plans) - 1
    width = x_ref.shape[1]
    quarter = width // 4
    third = down.shape[2] // 3

    def copies(s):
        return weight_copies(
            plans[s], pieces[s], gate_up.at[s], down.at[s], sems.at[s, 0], sems.at[s, 1]
        )

    @pl.when((step == 0) & (part == 0))
    def _():
        for s in range(len(plans)):
            wide, thin = copies(s)
            for copy in wide + thin:
                copy.start()

    for s in range(len(plans)):

        @pl.when((step == s) & (part == 0))
        def _():
            pltpu.make_async_copy(gate_up.at[s], gate_up.at[s], sems.at[s, 0]).wait()
            pltpu.make_async_copy(down.at[s], down.at[s], sems.at[s, 1]).wait()

    rows = pl.ds(pl.multiple_of(part * tile, tile), tile)
    act = dot(x_ref[rows, :], gate_up[step], 1, 0)
    for j, (gate, upper) in enumerate(split_act(act)):
        hid_ref[0, :, j * third : (j + 1) * third] = (gate * sigmoid(gate) * upper).astype(BF16)
    act_ref[0] = act.astype(BF16)
    grown = dot(hid_ref[0], down[step], 1, 1)

    @pl.when(step == 0)
    def _():
        total[rows, :] = in_ref[...] + grown

    @pl.when(step > 0)
    def _():
        total[rows, :] += grown

    @pl.when(step == final)
    def _():
        result = total[rows, :]
        if not last:
            sum_ref[...] = result
            return
        tok = x_ref.shape[0]
        slot = info[2] * tok + part * tile + lax.broadcasted_iota(jnp.int32, (tile, 1), 0)
        valid = jnp.where(slot < info[3], 1.0, 0.0)
        square = jnp.zeros((tile, quarter), F32)
        for p, mask in enumerate(MASKS):
            at = pl.multiple_of(jnp.bitwise_xor(info[1], mask) * quarter, quarter)
            cols = slice(p * quarter, (p + 1) * quarter)
            value = result[:, cols]
            low = value.astype(BF16)

            @pl.when(part < pl.num_programs(1) // 2)
            def _():
                outa_ref[:, pl.ds(at, quarter)] = low

            @pl.when(part >= pl.num_programs(1) // 2)
            def _():
                outb_ref[:, pl.ds(at, quarter)] = low

            error = valid * (value - teach_ref[0, :, pl.ds(at, quarter)].astype(F32))
            square = square + error * error
            grad = error * scale[0]
            gres_ref[:, cols] = grad
            low_ref[:, cols] = grad.astype(BF16)
            lowt_ref[cols, :] = grad.T.astype(BF16)

        @pl.when(part == 0)
        def _():
            sq_ref[...] = jnp.zeros_like(sq_ref)

        sq_ref[...] += jnp.sum(square, axis=0, keepdims=True)


def ffn_fwd(info, scale, x, total, teacher, weights, units, tile):
    tok, width = x.shape
    pieces = [piece for _, group in weights for piece in group]
    count = len(weights)
    last = teacher is not None
    entry = lambda s, i: jnp.where(s == 0, i, tok // tile - 1)
    leave = lambda s, i: jnp.where(s == count - 1, i, 0)
    tiles = lambda n: pl.BlockSpec((tile, n), lambda s, i, info: (leave(s, i), 0))
    slab = lambda n: pl.BlockSpec((1, tile, n), lambda s, i, info: (s, i, 0))
    in_specs = [
        SMEM,
        whole((tok, width)),
        pl.BlockSpec((tile, width), lambda s, i, info: (entry(s, i), 0)),
    ]
    out_specs = [slab(2 * units), slab(units)]
    out_shape = [shape_of((count, tok, 2 * units), BF16), shape_of((count, tok, units), BF16)]
    if last:
        in_specs.append(
            pl.BlockSpec((1, tile, width), lambda s, i, info: (info[0], leave(s, i), 0))
        )
        half = tok // tile // 2
        out_specs += [
            pl.BlockSpec(
                (tile, width), lambda s, i, info: (jnp.minimum(leave(s, i), half - 1), 0)
            ),
            pl.BlockSpec(
                (tile, width), lambda s, i, info: (jnp.maximum(leave(s, i) - half, 0), 0)
            ),
            tiles(width),
            tiles(width),
            pl.BlockSpec((width, tile), lambda s, i, info: (0, leave(s, i))),
            pl.BlockSpec((1, width // 4), lambda s, i, info: (0, 0)),
        ]
        out_shape += [
            shape_of((tok // 2, width), BF16),
            shape_of((tok // 2, width), BF16),
            shape_of((tok, width), F32),
            shape_of((tok, width), BF16),
            shape_of((width, tok), BF16),
            shape_of((1, width // 4), F32),
        ]
    else:
        out_specs.append(tiles(width))
        out_shape.append(shape_of((tok, width), F32))
    return pl.pallas_call(
        functools.partial(ffn_fwd_kernel, tile, [plan for plan, _ in weights], last),
        grid_spec=pltpu.PrefetchScalarGridSpec(
            num_scalar_prefetch=1,
            grid=(count, tok // tile),
            in_specs=in_specs + [ANY] * len(pieces),
            out_specs=out_specs,
            scratch_shapes=[
                pltpu.VMEM((count, width, 2 * units), BF16),
                pltpu.VMEM((count, width, units), BF16),
                pltpu.VMEM((tok, width), F32),
                pltpu.SemaphoreType.DMA((count, 2)),
            ],
        ),
        out_shape=out_shape,
        compiler_params=settings(2, 60),
        cost_estimate=cost(True),
        name="ffn_fwd",
    )(info, scale, x, total, *([teacher] if last else []), *pieces)


def ffn_bwd_kernel(steps, plan, first, low_ref, act_ref, hid_ref, xt_ref, lowt_ref, *rest):
    count = 1 + max(place[0] for chunks in plan for place in chunks)
    pieces, rest = rest[:count], rest[count:]
    if not first:
        in_ref, rest = rest[0], rest[1:]
    out_ref, keep_ref, send_ref, gate_up, down, dact_all, hid_all, sems = rest
    step = pl.program_id(0)
    units = down.shape[1]
    third = units // 3
    tile = low_ref.shape[0]

    @pl.when(step == 0)
    def _():
        wide, thin = weight_copies(plan, pieces, gate_up, down, sems.at[0], sems.at[1])
        for copy in thin + wide:
            copy.start()
        pltpu.make_async_copy(down, down, sems.at[1]).wait()

    @pl.when(step < steps)
    def _():
        rows = pl.ds(pl.multiple_of(step * tile, tile), tile)
        grad_hidden = dot(low_ref[...], down[...], 1, 0)
        for j, (gate, upper) in enumerate(split_act(act_ref[0])):
            grad = grad_hidden[:, j * third : (j + 1) * third]
            gate, upper = gate.astype(F32), upper.astype(F32)
            sig = sigmoid(gate)
            silu = gate * sig
            at = 2 * j * third
            dact_all[rows, at : at + third] = (
                grad * upper * (sig + silu - silu * sig)
            ).astype(BF16)
            dact_all[rows, at + third : at + 2 * third] = (grad * silu).astype(BF16)
        hid_all[rows, :] = hid_ref[0]

        @pl.when(step == 0)
        def _():
            pltpu.make_async_copy(gate_up, gate_up, sems.at[0]).wait()

        grown = dot(dact_all[rows, :], gate_up[...], 1, 1)
        out_ref[...] = grown if first else in_ref[...] + grown

    def weight_rows(target):
        target[:, : 2 * units] = dot(xt_ref[...], dact_all[...], 1, 0).astype(BF16)
        target[:, 2 * units :] = dot(lowt_ref[...], hid_all[...], 1, 0).astype(BF16)

    @pl.when((step >= steps) & (step < steps + 2))
    def _():
        weight_rows(send_ref)

    @pl.when(step >= steps + 2)
    def _():
        weight_rows(keep_ref)


def ffn_bwd(low, saved, weights, total, xt, lowt, tile):
    plan, pieces = weights
    acts, hiddens, block = saved
    tok, width = low.shape
    units = hiddens.shape[2]
    steps = tok // tile
    quarter = width // 4
    first = total is None
    clip = lambda i: jnp.minimum(i, steps - 1)
    rows_of = lambda n: pl.BlockSpec((tile, n), lambda i: (clip(i), 0))
    slab = lambda n: pl.BlockSpec((1, tile, n), lambda i: (block, clip(i), 0))
    feature = lambda i: (jnp.where(i < steps + 2, jnp.maximum(i - steps, 0) + 2, i - steps - 2), 0)
    return pl.pallas_call(
        functools.partial(ffn_bwd_kernel, steps, plan, first),
        grid=(steps + 4,),
        in_specs=[
            rows_of(width),
            slab(2 * units),
            slab(units),
            pl.BlockSpec((quarter, tok), feature),
            pl.BlockSpec((quarter, tok), feature),
        ]
        + [ANY] * len(pieces)
        + ([] if first else [rows_of(width)]),
        out_specs=[
            rows_of(width),
            pl.BlockSpec((quarter, 3 * units), lambda i: (jnp.maximum(i - steps - 2, 0), 0)),
            pl.BlockSpec((quarter, 3 * units), lambda i: (jnp.clip(i - steps, 0, 1), 0)),
        ],
        out_shape=[
            shape_of((tok, width), F32),
            shape_of((width // 2, 3 * units), BF16),
            shape_of((width // 2, 3 * units), BF16),
        ],
        scratch_shapes=[
            pltpu.VMEM((width, 2 * units), BF16),
            pltpu.VMEM((width, units), BF16),
            pltpu.VMEM((tok, 2 * units), BF16),
            pltpu.VMEM((tok, units), BF16),
            pltpu.SemaphoreType.DMA((2,)),
        ],
        input_output_aliases={} if first else {5 + len(pieces): 0},
        compiler_params=settings(1, 60),
        cost_estimate=cost(True),
        name="ffn_bwd",
    )(low, acts, hiddens, xt, lowt, *pieces, *([] if first else [total]))


def turn_chunks(block):
    wide = block.shape[1] * 2 // 9
    thin = wide // 2
    starts = [(2 * wide, wide), (wide, wide), (0, wide)]
    starts += [(3 * wide + 2 * thin, thin), (3 * wide + thin, thin), (3 * wide, thin)]
    return jnp.concatenate([block[:, a : a + n] for a, n in starts], axis=1)


def sum_kernel(turns, *refs):
    total = None
    for ref, turn in zip(refs[:-1], turns):
        value = ref[...].astype(F32)
        value = turn_chunks(value) if turn else value
        total = value if total is None else total + value
    refs[-1][...] = total.astype(refs[-1].dtype)


def summed(terms, turns=None, dtype=BF16):
    rows, cols = terms[0].shape
    spec = pl.BlockSpec((128, cols), lambda i: (i, 0))
    return pl.pallas_call(
        functools.partial(sum_kernel, turns or [False] * len(terms)),
        grid=(rows // 128,),
        in_specs=[spec] * len(terms),
        out_specs=spec,
        out_shape=shape_of((rows, cols), dtype),
        compiler_params=settings(1, 24),
        cost_estimate=cost(False),
        name="summed",
    )(*terms)


def core_sum_kernel(info, left_ref, right_ref, *outs):
    total = (left_ref[...].astype(F32) + right_ref[...].astype(F32)).astype(BF16)
    block = pl.program_id(1)
    place = block // 2 * 2 + jnp.bitwise_xor(block % 2, info[2])
    for i, out in enumerate(outs):

        @pl.when(place == i)
        def _():
            out[...] = total


def core_sum(info, keep, came):
    groups, rows, cols = keep.shape
    spec = pl.BlockSpec((1, rows // 4, cols), lambda g, i, info: (g, i, 0))
    return pl.pallas_call(
        core_sum_kernel,
        grid_spec=pltpu.PrefetchScalarGridSpec(
            num_scalar_prefetch=1,
            grid=(groups, 4),
            in_specs=[spec] * 2,
            out_specs=[pl.BlockSpec((1, rows // 4, cols), lambda g, i, info: (g, 0, 0))] * 4,
        ),
        out_shape=[shape_of((groups, rows // 4, cols), BF16)] * 4,
        compiler_params=settings(2, 24),
        cost_estimate=cost(False),
        name="core_sum",
    )(info, keep, came)


def weight_grad_kernel(nt_ref, back0_ref, back1_ref, gt_ref, att_ref, keep_ref, send_ref):
    cols = back0_ref.shape[2]
    part, block = pl.program_id(0), pl.program_id(1)

    def rows(target, back_ref):
        target[0, :, :cols] = dot(nt_ref[...], back_ref[0], 1, 0).astype(BF16)
        target[0, :, cols:] = dot(gt_ref[...], att_ref[0], 1, 0).astype(BF16)

    for j, back_ref in enumerate((back0_ref, back1_ref)):

        @pl.when((part == 0) & (block % 2 == j))
        def _():
            rows(send_ref, back_ref)

        @pl.when((part == 1) & (block % 2 == j))
        def _():
            rows(keep_ref, back_ref)


def weight_grad(normed_t, backs, grad_t, attended):
    width, tok = normed_t.shape
    cols, feats = backs[0].shape[2], attended.shape[2]
    half = pl.BlockSpec((width // 2, tok), lambda p, k: (1 - p, 0))
    side = pl.BlockSpec((1, tok, cols), lambda p, k: (k // 2, 0, 0))
    shape = (1, width // 2, cols + feats)
    return pl.pallas_call(
        weight_grad_kernel,
        grid=(2, 4),
        in_specs=[half, side, side, half, pl.BlockSpec((1, tok, feats), lambda p, k: (k, 0, 0))],
        out_specs=[
            pl.BlockSpec(shape, lambda p, k: (jnp.where(p == 0, 0, k), 0, 0)),
            pl.BlockSpec(shape, lambda p, k: (jnp.where(p == 0, k, 3), 0, 0)),
        ],
        out_shape=[shape_of((4, width // 2, cols + feats), BF16)] * 2,
        compiler_params=settings(2, 32),
        cost_estimate=cost(True),
        name="weight_grad",
    )(normed_t, *backs, grad_t, attended)


def after(value, *others):
    return lax.optimization_barrier((value,) + others)[0]


def per_device_rows(
    tokens,
    teacher,
    lengths,
    attn_gain,
    q_weight,
    k_weight,
    v_weight,
    q_gain,
    k_gain,
    o_weight,
    ffn_gain,
    gate_weight,
    up_weight,
    down_weight,
):
    z = lax.axis_index("tp")
    ctx = lax.axis_index("ctx")
    fsdp = lax.axis_index("fsdp")
    rows_dev, tok, width = tokens.shape
    quarter = width // 4
    hd = q_gain.shape[0] * 4
    q_cols, k_cols = q_weight.shape[1], k_weight.shape[1]
    proj = q_cols + 2 * k_cols
    heads = (q_cols // hd, k_cols // hd)
    units = gate_weight.shape[1]
    slots = rows_dev * 4 * tok * 2

    def x_swap(v):
        return lax.ppermute(v, "fsdp", X_SWAP)

    def core_swap(v):
        return lax.ppermute(v, "fsdp", CORE_SWAP)

    def y_swap(v):
        return lax.ppermute(v, "ctx", Y_SWAP)

    def z_up(v):
        return lax.ppermute(v, "tp", Z_UP)

    def z_far(v):
        return lax.ppermute(v, "tp", Z_FAR)

    def z_down(v):
        return lax.ppermute(v, "tp", Z_DOWN)

    def chunks(block):
        return [block[:, j * units : (j + 1) * units] for j in range(3)]

    def natural(v):
        v = jnp.concatenate([v[0:1], v[2:3], v[1:2], v[3:4]], axis=0)
        v = jnp.where(fsdp % 2 == 0, v, jnp.concatenate([v[1:2], v[0:1], v[3:4], v[2:3]], axis=0))
        return jnp.where(fsdp // 2 == 0, v, jnp.concatenate([v[2:4], v[0:2]], axis=0))

    v = {}

    def sync():
        v.update(lax.optimization_barrier(dict(v)))

    length = lax.dynamic_slice_in_dim(lengths, z, 1, 0)
    info = jnp.concatenate([jnp.stack([z, fsdp, ctx]).astype(jnp.int32), length])
    w_proj = join(q_weight, k_weight, v_weight)
    proj_z = [z_up(w_proj), z_far(w_proj), z_down(w_proj)]
    proj_far = x_swap(w_proj)
    count_here = jnp.sum(lengths).astype(F32)[None]
    vector = jnp.concatenate([attn_gain, ffn_gain, q_gain, k_gain]).astype(F32)
    vector = jnp.concatenate([vector, count_here, jnp.zeros((640 - 545,), F32)])[None]
    vector = jnp.concatenate([vector, x_swap(vector)], axis=0)
    vector = jnp.concatenate([vector, core_swap(vector)], axis=0)
    w_out, w_ffn = pack(info, o_weight, gate_weight, up_weight, down_weight)
    pos = (ctx * tok + jnp.arange(tok, dtype=jnp.int32)).astype(F32)
    frequency = THETA ** (-(2.0 * jnp.arange(hd // 2, dtype=F32)) / hd)
    angles = frequency[:, None] * pos[None, :]
    head_gains = natural(vector[:, 2 * quarter : 544])
    v.update(
        info=info,
        w_proj=w_proj,
        proj_far=proj_far,
        proj_z=jnp.concatenate(proj_z, axis=0),
        w_out=w_out,
        w_ffn=w_ffn,
        gain_one=vector[:, :quarter].reshape(1, width),
        gain_two=vector[:, quarter : 2 * quarter].reshape(1, width),
        total_count=jnp.sum(vector[:, 544]),
        gain_q=head_gains[:, : hd // 4].reshape(hd, 1),
        gain_k=head_gains[:, hd // 4 :].reshape(hd, 1),
        cos_part=jnp.cos(angles),
        sin_part=jnp.sin(angles),
    )
    sync()
    info = v["info"]

    proj_zfar = x_swap(v["proj_z"])
    out_z = [z_up(v["w_out"]), z_far(v["w_out"]), z_down(v["w_out"])]
    proj_core = core_swap(v["w_proj"])
    x_in, normed_one_t = norm_one(info, tokens, v["gain_one"], 256)
    v.update(
        proj_zfar=proj_zfar, proj_core=proj_core, x_in=x_in, normed_one_t=normed_one_t, out_z=out_z
    )
    sync()

    proj_cores = [v["proj_core"], core_swap(v["proj_far"])]
    proj_cores += [core_swap(v["proj_z"]), core_swap(v["proj_zfar"])]
    plan_proj = [[(0, 0), (1, 0), (4, 0), (5, 0)]]
    plan_proj += [[(p, k * quarter) for p in (2, 3, 6, 7)] for k in range(3)]
    weights_proj = [v["w_proj"], v["proj_far"], v["proj_z"], v["proj_zfar"]] + proj_cores
    ffn_one = z_up(v["w_ffn"])
    ffn_far = x_swap(v["w_ffn"])
    tables = [v[name] for name in ("cos_part", "sin_part", "gain_q", "gain_k")]

    def make(block, *then):
        normed_t = after(v["normed_one_t"], *then)
        return project(info, (plan_proj, weights_proj), normed_t, *tables, heads, block)

    theirs = [make(lambda s: 2 * (1 - s[2]))]
    got = [y_swap(theirs[0][0])]
    theirs.append(make(lambda s: 2 * (1 - s[2]) + 1, theirs[0][0]))
    got.append(y_swap(theirs[1][0]))
    mine = [make(lambda s: 2 * s[2], theirs[1][0])]
    mine.append(make(lambda s: 2 * s[2] + 1, mine[0][0]))
    v.update(
        ffn_one=ffn_one,
        ffn_far=ffn_far,
        weights_proj=weights_proj,
        mine=mine,
        theirs=theirs,
        got0=got[0],
    )
    sync()

    out_blocks = jnp.concatenate([v["w_out"]] + v["out_z"], axis=0)
    one_far = [x_swap(chunks(v["ffn_one"])[0])]
    three = [z_down(chunks(v["w_ffn"])[0])]
    own_cores = [core_swap(v["w_ffn"]), core_swap(v["ffn_far"])]
    first = attn_fwd(info, v["mine"][0][0], v["got0"], hd)
    v.update(
        first=first,
        got1=got[1],
        one_far=one_far,
        three=three,
        out_blocks=out_blocks,
        own_cores=own_cores,
    )
    sync()

    arrived = [y_swap(v["first"][1])]
    three = v["three"] + [z_down(chunks(v["w_ffn"])[1])]
    out_far = x_swap(v["out_blocks"])
    one_cores = [core_swap(v["ffn_one"]), core_swap(v["one_far"][0])]
    second = attn_fwd(info, v["mine"][1][0], v["got1"], hd)
    v.update(second=second, arrived=arrived, three=three, out_far=out_far, one_cores=one_cores)
    sync()

    arrived = v["arrived"] + [y_swap(v["second"][1])]
    three = v["three"] + [z_down(chunks(v["w_ffn"])[2])]
    one_far = v["one_far"] + [x_swap(chunks(v["ffn_one"])[1])]
    weights_out = [v["out_blocks"], v["out_far"]]
    weights_out += [core_swap(v["out_blocks"]), core_swap(v["out_far"])]
    v.update(arrived=arrived, three=three, one_far=one_far, weights_out=weights_out)
    sync()

    plan_out = [[(p, k * quarter) for p in range(4)] for k in range(4)]
    two = [z_up(chunks(v["ffn_one"])[0])]
    three_far = [x_swap(v["three"][0])]
    one_last = y_swap(v["one_far"][0])
    one_cores = v["one_cores"] + [core_swap(v["one_far"][1])]
    resid, normed_two, normed_two_t, attended = out_proj(
        info,
        v["x_in"],
        [v["first"][0], v["second"][0]],
        v["arrived"],
        (plan_out, v["weights_out"]),
        v["gain_two"],
        256,
    )
    v.update(
        two=two,
        three_far=three_far,
        one_last=one_last,
        one_cores=one_cores,
        resid=resid,
        normed_two=normed_two,
        normed_two_t=normed_two_t,
        attended=attended,
    )
    sync()

    in_block = lambda i: [(i, 0, j * units) for j in range(3)]
    plan0 = [in_block(i) for i in range(4)]
    plan1 = [in_block(0), [(i, 0, 0) for i in (1, 2, 3)]]
    plan1 += [in_block(4), [(i, 0, 0) for i in (5, 6, 7)]]
    plan3 = [[(0, 0, 0), (1, 0, 0), (2, 0, 0)], [(3, 0, 0), (4, 0, 0), (5, 0, 0)]]
    plan3 += [[(6, j * quarter, 0) for j in range(3)]]
    plan3 += [[(6, 3 * quarter, 0), (7, 0, 0), (8, 0, 0)]]
    plan2 = [[(0, 0, 0), (1, 0, 0), (1, 0, units)], [(2, quarter, 0), (3, 0, 0), (4, 0, 0)]]
    plan2 += [[(5, 4 * quarter, 0), (6, 0, 0), (6, 0, units)]]
    plan2 += [[(7, quarter, 0), (8, 0, 0), (9, 0, 0)]]
    scale = (slots / v["total_count"])[None]
    weights0 = [v["w_ffn"], v["ffn_far"]] + v["own_cores"]
    weights1 = [v["ffn_one"]] + v["one_far"] + [v["one_last"]]
    weights1 += v["one_cores"] + [core_swap(v["one_last"])]
    two = v["two"] + [z_up(v["ffn_one"][:, units:])]
    mixed_far = x_swap(jnp.concatenate([v["three"][1], v["two"][0]], axis=0))
    three_last = y_swap(v["three_far"][0])
    mixed = jnp.concatenate(v["three"] + [v["three_far"][0], v["two"][0]], axis=0)
    mixed_core = core_swap(mixed)
    acts_a, hiddens_a, sum_a = ffn_fwd(
        info,
        scale,
        after(v["normed_two"], mixed),
        v["resid"],
        None,
        [(plan0, weights0), (plan1, weights1)],
        units,
        256,
    )
    v.update(
        scale=scale,
        weights0=weights0,
        weights1=weights1,
        two=two,
        mixed_far=mixed_far,
        three_last=three_last,
        mixed_core=mixed_core,
        acts_a=acts_a,
        hiddens_a=hiddens_a,
        sum_a=sum_a,
    )
    sync()

    far_core = core_swap(v["mixed_far"])
    weights3 = v["three"] + [v["three_far"][0], v["mixed_far"], v["three_last"]]
    weights3 += [v["mixed_core"], far_core, core_swap(v["three_last"])]
    two_far = x_swap(v["two"][1][:, :units])
    two_last = y_swap(v["mixed_far"][quarter:])
    two_core = core_swap(v["two"][1])
    acts_b, hiddens_b, sum_b = ffn_fwd(
        info, v["scale"], v["normed_two"], v["sum_a"], None, [(plan3, weights3)], units, 256
    )
    v.update(
        weights3=weights3,
        far_core=far_core,
        two_far=two_far,
        two_last=two_last,
        two_core=two_core,
        acts_b=acts_b,
        hiddens_b=hiddens_b,
        sum_b=sum_b,
    )
    sync()

    weights2 = v["two"] + [v["mixed_far"], v["two_far"], v["two_last"]]
    weights2 += [v["mixed_core"], v["two_core"], v["far_core"]]
    weights2 += [core_swap(v["two_far"]), core_swap(v["two_last"])]
    acts_c, hiddens_c, *results, grad_result, grad_low, grad_low_t, square = ffn_fwd(
        info, v["scale"], v["normed_two"], v["sum_b"], teacher, [(plan2, weights2)], units, 256
    )
    v.update(
        weights2=weights2,
        acts_c=acts_c,
        hiddens_c=hiddens_c,
        results=results,
        grad_result=grad_result,
        grad_low=grad_low,
        grad_low_t=grad_low_t,
        square=square,
    )
    sync()

    def ffn_back(plan, weights, acts, hiddens, block, total):
        return ffn_bwd(
            v["grad_low"],
            (v[acts], v[hiddens], block),
            (plan, v[weights]),
            total,
            v["normed_two_t"],
            v["grad_low_t"],
            256,
        )

    def sum_of(k):
        return [p[0] for p in core_sum(info, v[f"keep{k}"][None], v[f"came{k}"][None])]

    turned = [False, False, True]
    one = [z_up(v["results"][0])]
    total, keep2, send2 = ffn_back(plan2, "weights2", "acts_c", "hiddens_c", 0, None)
    v.update(one=one, total=total, keep2=keep2, send2=send2)
    sync()

    one = v["one"] + [z_up(v["results"][1])]
    came2 = core_swap(v["send2"])
    total, keep1, send1 = ffn_back(plan1, "weights1", "acts_a", "hiddens_a", 1, v["total"])
    v.update(one=one, came2=came2, total=total, keep1=keep1, send1=send1)
    sync()

    out_three = [z_down(v["results"][0])]
    came1 = core_swap(v["send1"])
    sum2 = sum_of(2)
    far_t2 = x_swap(sum2[3])
    total, keep3, send3 = ffn_back(
        plan3, "weights3", "acts_b", "hiddens_b", 0, after(v["total"], sum2[0])
    )
    v.update(
        out_three=out_three,
        came1=came1,
        sum2=sum2,
        far_t2=far_t2,
        total=total,
        keep3=keep3,
        send3=send3,
    )
    sync()

    out_three = v["out_three"] + [z_down(v["results"][1])]
    came3 = core_swap(v["send3"])
    far_h2 = x_swap(v["sum2"][2])
    there2 = y_swap(summed([v["sum2"][1], v["far_t2"]]))
    sum1 = sum_of(1)
    total, keep0, send0 = ffn_back(
        plan0, "weights0", "acts_a", "hiddens_a", 0, after(v["total"], sum1[0])
    )
    v.update(
        out_three=out_three,
        came3=came3,
        far_h2=far_h2,
        there2=there2,
        sum1=sum1,
        total=total,
        keep0=keep0,
        send0=send0,
    )
    sync()

    came0 = core_swap(v["send0"])
    far_t1 = x_swap(v["sum1"][3])
    down2 = z_down(summed([v["sum2"][0], v["far_h2"], v["there2"]], turned))
    sum3 = sum_of(3)
    grad_resid, grad_attn_t, a0, a1, b0, b1, gain_two_sum = norm_two_back(
        info,
        after(v["total"], sum3[0]),
        v["resid"],
        v["grad_result"],
        v["gain_two"],
        (plan_out, v["weights_out"]),
        256,
    )
    grad_got = [y_swap(b0), y_swap(b1)]
    v.update(
        came0=came0,
        far_t1=far_t1,
        down2=down2,
        sum3=sum3,
        grad_resid=grad_resid,
        grad_attn_t=grad_attn_t,
        grad_mine=[a0, a1],
        gain_two_sum=gain_two_sum,
        grad_got0=grad_got[0],
    )
    sync()

    def attn_back(j, grad):
        out, got_ref = v["first" if j == 0 else "second"], v[f"got{j}"]
        return attn_bwd(
            info, v["mine"][j][0], got_ref, out[0], out[1], grad, v[f"grad_got{j}"], out[2], hd
        )

    two = [z_up(v["one"][0])]
    far_h1 = x_swap(v["sum1"][2])
    there1 = y_swap(summed([v["sum1"][1], v["far_t1"]]))
    far_t3 = x_swap(v["sum3"][3])
    sum0 = sum_of(0)
    back0 = attn_back(0, after(v["grad_mine"][0], sum0[0]))
    v.update(
        out_two=two,
        far_h1=far_h1,
        there1=there1,
        far_t3=far_t3,
        sum0=sum0,
        back0=back0,
        grad_got1=grad_got[1],
    )
    sync()

    two = v["out_two"] + [z_up(v["one"][1])]
    heads0 = y_swap(v["back0"][1])
    far_h3 = x_swap(v["sum3"][2])
    far_t0 = x_swap(v["sum0"][3])
    there3 = summed([v["sum3"][1], v["far_t3"]])
    two_down = summed(
        [v["sum1"][0], v["far_h1"], v["there1"], v["down2"]], [False, False, True, False]
    )
    there3_got = y_swap(there3)
    two_down_got = z_down(two_down)
    back1 = attn_back(1, after(v["grad_mine"][1], there3, two_down))
    v.update(
        out_two=two, heads0=heads0, far_h3=far_h3, far_t0=far_t0, there3=there3_got, back1=back1
    )
    sync()

    heads1 = y_swap(v["back1"][1])
    far_h0 = x_swap(v["sum0"][2])
    up3 = z_up(summed([v["sum3"][0], v["far_h3"], v["there3"]], turned))
    tables = [v[name] for name in ("cos_part", "sin_part", "gain_q", "gain_k")]
    head0 = head_back(
        info, v["back0"][0], v["heads0"], v["mine"][0][1], v["theirs"][0][1], *tables, heads
    )
    v.update(heads1=heads1, two_down=two_down_got, head0=head0)
    sync()

    there0 = y_swap(summed([v["sum0"][1], v["far_t0"]]))
    head1 = head_back(
        info, v["back1"][0], v["heads1"], v["mine"][1][1], v["theirs"][1][1], *tables, heads
    )
    *tokens_low, gain_one_sum = norm_one_back(
        info,
        [v["head0"][0], head1[0]],
        (plan_proj, v["weights_proj"]),
        v["x_in"],
        v["grad_resid"],
        v["gain_one"],
        256,
    )
    v.update(head1=head1, tokens_low=tokens_low, gain_one_sum=gain_one_sum, up3=up3)
    sync()

    tok_one = [z_up(v["tokens_low"][0])]
    keep, send = weight_grad(
        v["normed_one_t"], [v["head0"][0], v["head1"][0]], v["grad_attn_t"], v["attended"]
    )
    v.update(tok_one=tok_one, keep=keep, send=send, there0=there0, far_h0=far_h0)
    sync()

    tok_one = v["tok_one"] + [z_up(v["tokens_low"][1])]
    tok_three = [z_down(v["tokens_low"][0])]
    rows = quarter // 2
    flat = lambda a: a.reshape(4 * rows, a.shape[-1])
    sums = [flat(p) for p in core_sum(info, v["keep"], core_swap(v["send"]))]
    far_t = x_swap(sums[3])
    far_h = x_swap(sums[2])
    part0 = summed([v["sum0"][0], v["far_h0"], v["there0"]], turned)
    ffn_sum = summed([part0, v["two_down"], v["up3"]], None, F32)
    v.update(sums=sums[:2], far_t=far_t, ffn_sum=ffn_sum, tok_one=tok_one)
    sync()

    tok_three.append(z_down(v["tokens_low"][1]))
    there = y_swap(summed([v["sums"][1], v["far_t"]]))
    ffn_other = y_swap(v["ffn_sum"])
    v.update(tok_three=tok_three, there=there, far_h=far_h)
    sync()

    parts = summed([v["sums"][0], v["far_h"], v["there"]])
    parts = [parts[k * rows : (k + 1) * rows] for k in range(4)]
    parts = [parts[0], z_down(parts[1]), z_far(parts[2]), z_up(parts[3])]
    tok_two = [z_up(v["tok_one"][0])]
    v.update(parts=parts, ffn_other=ffn_other, tok_two=tok_two)
    sync()

    attn_sum = summed(v["parts"], None, F32)
    attn_other = y_swap(attn_sum)
    tok_two = v["tok_two"] + [z_up(v["tok_one"][1])]

    def spread(own, one, two, three, dtype):
        out = jnp.zeros((rows_dev, tok, width), dtype)
        for k, parts in ((0, own), (1, one), (3, three), (2, two)):
            row = lax.rem(z - k + 4, 4)
            for j, part in enumerate(parts):
                out = lax.dynamic_update_slice(
                    out, part.astype(dtype)[None], (row, j * tok // 2, 0)
                )
        return out

    tokens_grad = spread(v["tokens_low"], v["tok_one"], tok_two, v["tok_three"], F32)
    output = spread(v["results"], v["one"], v["out_two"], v["out_three"], BF16)

    def finish(own, other):
        return jnp.concatenate(
            [jnp.where(ctx == 0, own, other), jnp.where(ctx == 0, other, own)], axis=0
        )

    ffn_grad = finish(v["ffn_sum"], turn_chunks(v["ffn_other"]))
    attn_grad = finish(attn_sum, attn_other)

    def total(v):
        for axis, pairs in (("fsdp", CORE_SWAP), ("fsdp", X_SWAP), ("ctx", Y_SWAP)):
            v = v + lax.ppermute(v, axis, pairs)
        for pairs in (Z_NEAR, Z_FAR):
            v = v + lax.ppermute(v, "tp", pairs)
        return v

    back = [v["head0"], v["head1"]]
    gain_one_sum, gain_two_sum, square = v["gain_one_sum"], v["gain_two_sum"], v["square"]
    total_count = v["total_count"]
    gain_heads = back[0][1] + back[1][1]
    sums = total(
        jnp.concatenate(
            [
                natural(gain_one_sum.reshape(4, quarter)).reshape(1, width),
                natural(gain_two_sum.reshape(4, quarter)).reshape(1, width),
                gain_heads[:, 0].reshape(1, hd),
                gain_heads[:, 1].reshape(1, hd),
                jnp.sum(square).reshape(1, 1),
                jnp.zeros((1, 127), F32),
            ],
            axis=1,
        )
    )[0]
    teacher_loss = sums[2 * width + 2 * hd] / (total_count * width)

    def own_part(at, size):
        return lax.dynamic_slice_in_dim(sums, at + fsdp * (size // 4), size // 4, 0)

    third = units // 3

    def columns(first):
        starts = [first(j) for j in range(3)]
        parts = [ffn_grad[:, s : s + third] for s in starts]
        return jnp.concatenate(
            [jnp.where(ctx == 0, parts[0], parts[2]), parts[1], jnp.where(ctx == 0, parts[2], parts[0])],
            axis=1,
        )

    return (
        output,
        teacher_loss,
        tokens_grad,
        own_part(0, width),
        attn_grad[:, :q_cols],
        attn_grad[:, q_cols : q_cols + k_cols],
        attn_grad[:, q_cols + k_cols : proj],
        own_part(2 * width, hd),
        own_part(2 * width + hd, hd),
        attn_grad[:, proj:].T,
        own_part(width, width),
        columns(lambda j: 2 * j * third),
        columns(lambda j: (2 * j + 1) * third),
        columns(lambda j: 2 * units + j * third).T,
    )


def solution(mesh):
    return jax.shard_map(
        per_device_rows if fits(mesh) else per_device_any,
        mesh=mesh,
        in_specs=(
            P("fsdp", "ctx", None),
            P("fsdp", "ctx", None),
            P("fsdp"),
            P("fsdp"),
            P("fsdp", "tp"),
            P("fsdp", "tp"),
            P("fsdp", "tp"),
            P("fsdp"),
            P("fsdp"),
            P("tp", "fsdp"),
            P("fsdp"),
            P("fsdp", "tp"),
            P("fsdp", "tp"),
            P("tp", "fsdp"),
        ),
        out_specs=(
            P("fsdp", "ctx", None),
            P(),
            P("fsdp", "ctx", None),
            P("fsdp"),
            P("fsdp", "tp"),
            P("fsdp", "tp"),
            P("fsdp", "tp"),
            P("fsdp"),
            P("fsdp"),
            P("tp", "fsdp"),
            P("fsdp"),
            P("fsdp", "tp"),
            P("fsdp", "tp"),
            P("tp", "fsdp"),
        ),
        check_vma=False,
    )
```

```python
import functools
import math

import jax
import jax.numpy as jnp
from jax import lax
from jax.experimental import pallas as pl
from jax.experimental.pallas import tpu as pltpu
from jax.sharding import PartitionSpec as P

EPS = 1e-05
THETA = 1000000.0
NEGATIVE = -1e30


def rms_scale(field_in, gain_vec):
    return (
        field_in * lax.rsqrt(jnp.mean(field_in * field_in, axis=-1, keepdims=True) + EPS) * gain_vec
    )


def rotate(field_in, positions):
    half_dim = field_in.shape[-1] // 2
    frequency = THETA ** (-(2.0 * jnp.arange(half_dim, dtype=jnp.float32)) / field_in.shape[-1])
    angles = positions[:, None] * frequency[None, :]
    cos_part = jnp.cos(angles)[:, None, :]
    sin_part = jnp.sin(angles)[:, None, :]
    lower_half = field_in[..., :half_dim]
    upper_half = field_in[..., half_dim:]
    return jnp.concatenate(
        [
            lower_half * cos_part - upper_half * sin_part,
            upper_half * cos_part + lower_half * sin_part,
        ],
        axis=-1,
    )


def linear(left_mat, right_mat):
    return jnp.dot(left_mat, right_mat, preferred_element_type=jnp.float32)


def linear_left(left_mat, right_mat):
    return lax.dot_general(
        left_mat, right_mat, (((0,), (0,)), ((), ())), preferred_element_type=jnp.float32
    )


def linear_right(left_mat, right_mat):
    return lax.dot_general(
        left_mat, right_mat, (((1,), (1,)), ((), ())), preferred_element_type=jnp.float32
    )


def swiglu(gate_act, up_act):
    return jax.nn.silu(gate_act) * up_act


def per_device_any(
    tokens,
    teacher,
    lengths,
    attn_gain,
    q_weight,
    k_weight,
    v_weight,
    q_gain,
    k_gain,
    o_weight,
    ffn_gain,
    gate_weight,
    up_weight,
    down_weight,
):
    (
        gain_one,
        w_query,
        w_key,
        w_value,
        gain_query,
        gain_key,
        w_output,
        gain_two,
        w_gate,
        w_upper,
        w_down,
    ) = (
        lax.all_gather(attn_gain, "fsdp", axis=0, tiled=True),
        lax.all_gather(q_weight, "fsdp", axis=0, tiled=True),
        lax.all_gather(k_weight, "fsdp", axis=0, tiled=True),
        lax.all_gather(v_weight, "fsdp", axis=0, tiled=True),
        lax.all_gather(q_gain, "fsdp", axis=0, tiled=True),
        lax.all_gather(k_gain, "fsdp", axis=0, tiled=True),
        lax.all_gather(o_weight, "fsdp", axis=1, tiled=True),
        lax.all_gather(ffn_gain, "fsdp", axis=0, tiled=True),
        lax.all_gather(gate_weight, "fsdp", axis=0, tiled=True),
        lax.all_gather(up_weight, "fsdp", axis=0, tiled=True),
        lax.all_gather(down_weight, "fsdp", axis=1, tiled=True),
    )
    rows_dev, block_len, model_width = tokens.shape
    count_tok = rows_dev * block_len
    head_dim = gain_query.shape[0]
    q_heads = w_query.shape[1] // head_dim
    kv_heads = w_key.shape[1] // head_dim
    group_size = q_heads // kv_heads
    score_scale = head_dim ** (-0.5)
    row_len = block_len * lax.axis_size("ctx")
    key_block = math.gcd(row_len, 512)
    block_start = lax.axis_index("ctx") * block_len
    tiles_used = (block_start + block_len + key_block - 1) // key_block
    slot_pos = block_start + jnp.arange(block_len, dtype=jnp.int32)
    positions = slot_pos.astype(jnp.float32)
    valid = (slot_pos[None, :] < lengths[:, None]).astype(jnp.float32)
    slots = count_tok * lax.axis_size("fsdp") * lax.axis_size("ctx")
    gain_two_f = gain_two.astype(jnp.float32)
    gain_one_f = gain_one.astype(jnp.float32)
    inputs = tokens.astype(jnp.float32)
    normed_one, back_one = jax.vjp(rms_scale, inputs, gain_one_f)
    normed_low = normed_one.astype(jnp.bfloat16).reshape(count_tok, model_width)
    query_raw = linear(normed_low, w_query)
    key_raw = linear(normed_low, w_key)
    value_raw = linear(normed_low, w_value)

    def heads_post(raw_heads, gain_vec):
        shaped = raw_heads.reshape(rows_dev, block_len, -1, head_dim)
        return rotate(rms_scale(shaped, gain_vec), positions)

    query_rot, query_back = jax.vjp(heads_post, query_raw, gain_query.astype(jnp.float32))
    key_rot, key_back = jax.vjp(heads_post, key_raw, gain_key.astype(jnp.float32))
    queries = query_rot.astype(jnp.bfloat16).reshape(
        rows_dev, block_len, kv_heads, group_size, head_dim
    )
    key_rows = key_rot.astype(jnp.bfloat16).reshape(rows_dev, block_len, kv_heads * head_dim)
    values = value_raw.astype(jnp.bfloat16).reshape(rows_dev, block_len, kv_heads * head_dim)
    keys_all, values_all = (
        lax.all_gather(key_rows, "ctx", axis=1, tiled=True),
        lax.all_gather(values, "ctx", axis=1, tiled=True),
    )

    def key_tile(tile_index):
        tile_start = tile_index * key_block
        key_pos = tile_start + jnp.arange(key_block, dtype=jnp.int32)
        key_part = lax.dynamic_slice_in_dim(keys_all, tile_start, key_block, 1).reshape(
            rows_dev, key_block, kv_heads, head_dim
        )
        value_part = lax.dynamic_slice_in_dim(values_all, tile_start, key_block, 1).reshape(
            rows_dev, key_block, kv_heads, head_dim
        )
        scores = (
            jnp.einsum("rqhgd,rkhd->rhgqk", queries, key_part, preferred_element_type=jnp.float32)
            * score_scale
        )
        allowed = (key_pos[None, None, :] <= slot_pos[None, :, None]) & (
            key_pos[None, None, :] < lengths[:, None, None]
        )
        return (tile_start, scores, allowed[:, None, None], key_part, value_part)

    stat_shape = (rows_dev, kv_heads, group_size, block_len)

    def stats_step(tile_index, carried):
        running_max, running_sum = carried
        tile_start, scores, allowed, key_part, value_part = key_tile(tile_index)
        masked = jnp.where(allowed, scores, NEGATIVE)
        new_max = jnp.maximum(running_max, jnp.max(masked, axis=-1))
        terms = jnp.where(allowed, jnp.exp(masked - new_max[..., None]), 0.0)
        return (new_max, running_sum * jnp.exp(running_max - new_max) + jnp.sum(terms, axis=-1))

    running_max, running_sum = lax.fori_loop(
        0,
        tiles_used,
        stats_step,
        (jnp.full(stat_shape, NEGATIVE, jnp.float32), jnp.zeros(stat_shape, jnp.float32)),
    )
    log_total = running_max + jnp.log(running_sum)
    out_shape = (rows_dev, block_len, kv_heads, group_size, head_dim)

    def value_step(tile_index, carried):
        rounded_out, exact_out = carried
        tile_start, scores, allowed, key_part, value_part = key_tile(tile_index)
        tile_probs = jnp.where(allowed, jnp.exp(scores - log_total[..., None]), 0.0)
        rounded_out = rounded_out + jnp.einsum(
            "rhgqk,rkhd->rqhgd",
            tile_probs.astype(jnp.bfloat16),
            value_part,
            preferred_element_type=jnp.float32,
        )
        exact_out = exact_out + jnp.einsum(
            "rhgqk,rkhd->rqhgd", tile_probs, value_part.astype(jnp.float32)
        )
        return (rounded_out, exact_out)

    rounded_out, exact_out = lax.fori_loop(
        0,
        tiles_used,
        value_step,
        (jnp.zeros(out_shape, jnp.float32), jnp.zeros(out_shape, jnp.float32)),
    )
    attended = rounded_out.astype(jnp.bfloat16).reshape(count_tok, q_heads * head_dim)
    attn_total = lax.psum(linear(attended, w_output), "tp")
    resid = inputs + attn_total.reshape(rows_dev, block_len, model_width)
    normed_two, back_two = jax.vjp(rms_scale, resid, gain_two_f)
    normed_second = normed_two.astype(jnp.bfloat16).reshape(count_tok, model_width)
    gate_act = linear(normed_second, w_gate)
    up_act = linear(normed_second, w_upper)
    hidden_full, back_glu = jax.vjp(swiglu, gate_act, up_act)
    hidden = hidden_full.astype(jnp.bfloat16)
    ffn_total = lax.psum(linear(hidden, w_down), "tp")
    result = resid + ffn_total.reshape(rows_dev, block_len, model_width)
    error_value = result - teacher.astype(jnp.float32)
    valid_col = valid[..., None]
    total_square, total_count = lax.psum(
        (jnp.sum(valid_col * error_value * error_value), jnp.sum(valid)), ("fsdp", "ctx")
    )
    teacher_loss = total_square / (total_count * model_width)
    grad_result = valid_col * error_value * (slots / total_count)
    grad_low = grad_result.astype(jnp.bfloat16).reshape(count_tok, model_width)
    grad_down = linear_left(hidden, grad_low)
    grad_hidden = linear_right(grad_low, w_down)
    grad_gate_full, grad_up_full = back_glu(grad_hidden)
    grad_gate = grad_gate_full.astype(jnp.bfloat16)
    grad_up = grad_up_full.astype(jnp.bfloat16)
    grad_wgate = linear_left(normed_second, grad_gate)
    grad_wup = linear_left(normed_second, grad_up)
    normed_two_part = linear_right(grad_gate, w_gate) + linear_right(grad_up, w_upper)
    grad_normed_two = lax.psum(normed_two_part, "tp")
    grad_resid_norm, grad_gain_two = back_two(
        grad_normed_two.reshape(rows_dev, block_len, model_width)
    )
    grad_resid = grad_result + grad_resid_norm
    grad_attn_low = grad_resid.astype(jnp.bfloat16).reshape(count_tok, model_width)
    grad_woutput = linear_left(attended, grad_attn_low)
    grad_attended = linear_right(grad_attn_low, w_output).astype(jnp.bfloat16).reshape(out_shape)
    delta = jnp.einsum("rqhgd,rqhgd->rhgq", grad_attended.astype(jnp.float32), exact_out)
    full_shape = (rows_dev, row_len, kv_heads * head_dim)

    def grad_step(tile_index, carried):
        grad_queries, grad_keys, grad_values = carried
        tile_start, scores, allowed, key_part, value_part = key_tile(tile_index)
        tile_probs = jnp.where(allowed, jnp.exp(scores - log_total[..., None]), 0.0)
        grad_probs = jnp.einsum(
            "rqhgd,rkhd->rhgqk", grad_attended, value_part, preferred_element_type=jnp.float32
        )
        grad_scores = (tile_probs * (grad_probs - delta[..., None])).astype(jnp.bfloat16)
        grad_queries = (
            grad_queries
            + jnp.einsum(
                "rhgqk,rkhd->rqhgd", grad_scores, key_part, preferred_element_type=jnp.float32
            )
            * score_scale
        )
        key_term = (
            jnp.einsum(
                "rhgqk,rqhgd->rkhd", grad_scores, queries, preferred_element_type=jnp.float32
            )
            * score_scale
        )
        value_term = jnp.einsum(
            "rhgqk,rqhgd->rkhd",
            tile_probs.astype(jnp.bfloat16),
            grad_attended,
            preferred_element_type=jnp.float32,
        )
        grad_keys = lax.dynamic_update_slice_in_dim(
            grad_keys, key_term.reshape(rows_dev, key_block, kv_heads * head_dim), tile_start, 1
        )
        grad_values = lax.dynamic_update_slice_in_dim(
            grad_values, value_term.reshape(rows_dev, key_block, kv_heads * head_dim), tile_start, 1
        )
        return (grad_queries, grad_keys, grad_values)

    grad_queries, grad_keys, grad_values = lax.fori_loop(
        0,
        tiles_used,
        grad_step,
        (
            jnp.zeros(out_shape, jnp.float32),
            jnp.zeros(full_shape, jnp.float32),
            jnp.zeros(full_shape, jnp.float32),
        ),
    )
    key_grad, value_grad = (
        lax.psum_scatter(grad_keys, "ctx", scatter_dimension=1, tiled=True),
        lax.psum_scatter(grad_values, "ctx", scatter_dimension=1, tiled=True),
    )
    grad_query_raw, grad_gain_query = query_back(
        grad_queries.reshape(rows_dev, block_len, q_heads, head_dim)
    )
    grad_key_raw, grad_gain_key = key_back(
        key_grad.reshape(rows_dev, block_len, kv_heads, head_dim)
    )
    query_low = grad_query_raw.astype(jnp.bfloat16)
    key_low = grad_key_raw.astype(jnp.bfloat16)
    value_low = value_grad.reshape(count_tok, kv_heads * head_dim).astype(jnp.bfloat16)
    grad_wquery = linear_left(normed_low, query_low)
    grad_wkey = linear_left(normed_low, key_low)
    grad_wvalue = linear_left(normed_low, value_low)
    normed_part = (
        linear_right(query_low, w_query)
        + linear_right(key_low, w_key)
        + linear_right(value_low, w_value)
    )
    grad_normed_one, grad_gain_query, grad_gain_key = lax.psum(
        (normed_part, grad_gain_query, grad_gain_key), "tp"
    )
    grad_input_norm, grad_gain_one = back_one(
        grad_normed_one.reshape(rows_dev, block_len, model_width)
    )
    tokens_grad = grad_resid + grad_input_norm
    partials = (
        grad_gain_one,
        grad_wquery,
        grad_wkey,
        grad_wvalue,
        grad_gain_query,
        grad_gain_key,
        grad_woutput,
        grad_gain_two,
        grad_wgate,
        grad_wup,
        grad_down,
    )
    pieces = (
        lax.psum_scatter(partials[0], ("fsdp", "ctx"), scatter_dimension=0, tiled=True),
        lax.psum_scatter(partials[1], ("fsdp", "ctx"), scatter_dimension=0, tiled=True),
        lax.psum_scatter(partials[2], ("fsdp", "ctx"), scatter_dimension=0, tiled=True),
        lax.psum_scatter(partials[3], ("fsdp", "ctx"), scatter_dimension=0, tiled=True),
        lax.psum_scatter(partials[4], ("fsdp", "ctx"), scatter_dimension=0, tiled=True),
        lax.psum_scatter(partials[5], ("fsdp", "ctx"), scatter_dimension=0, tiled=True),
        lax.psum_scatter(partials[6], ("fsdp", "ctx"), scatter_dimension=1, tiled=True),
        lax.psum_scatter(partials[7], ("fsdp", "ctx"), scatter_dimension=0, tiled=True),
        lax.psum_scatter(partials[8], ("fsdp", "ctx"), scatter_dimension=0, tiled=True),
        lax.psum_scatter(partials[9], ("fsdp", "ctx"), scatter_dimension=0, tiled=True),
        lax.psum_scatter(partials[10], ("fsdp", "ctx"), scatter_dimension=1, tiled=True),
    )
    summed = (
        lax.all_gather(pieces[0], "ctx", axis=0, tiled=True),
        lax.all_gather(pieces[1], "ctx", axis=0, tiled=True),
        lax.all_gather(pieces[2], "ctx", axis=0, tiled=True),
        lax.all_gather(pieces[3], "ctx", axis=0, tiled=True),
        lax.all_gather(pieces[4], "ctx", axis=0, tiled=True),
        lax.all_gather(pieces[5], "ctx", axis=0, tiled=True),
        lax.all_gather(pieces[6], "ctx", axis=1, tiled=True),
        lax.all_gather(pieces[7], "ctx", axis=0, tiled=True),
        lax.all_gather(pieces[8], "ctx", axis=0, tiled=True),
        lax.all_gather(pieces[9], "ctx", axis=0, tiled=True),
        lax.all_gather(pieces[10], "ctx", axis=1, tiled=True),
    )
    return (
        result.astype(jnp.bfloat16),
        teacher_loss,
        tokens_grad,
        summed[0],
        summed[1],
        summed[2],
        summed[3],
        summed[4],
        summed[5],
        summed[6],
        summed[7],
        summed[8],
        summed[9],
        summed[10],
    )


BF16 = jnp.bfloat16
F32 = jnp.float32
LOG2E = math.log2(math.e)
X_SWAP = [(0, 2), (2, 0), (1, 3), (3, 1)]
CORE_SWAP = [(0, 1), (1, 0), (2, 3), (3, 2)]
Y_SWAP = [(0, 1), (1, 0)]
Z_UP = [(0, 1), (1, 2), (2, 3), (3, 0)]
Z_DOWN = [(0, 3), (1, 0), (2, 1), (3, 2)]
Z_NEAR = [(0, 1), (1, 0), (2, 3), (3, 2)]
Z_FAR = [(0, 2), (2, 0), (1, 3), (3, 1)]
MASKS = (0, 2, 1, 3)
ANY = pl.BlockSpec(memory_space=pl.ANY)
SMEM = pl.BlockSpec(memory_space=pltpu.SMEM)


def fits(mesh):
    return dict(mesh.shape) == {"fsdp": 4, "ctx": 2, "tp": 4}


def dot(left, right, left_dim, right_dim):
    return lax.dot_general(
        left, right, (((left_dim,), (right_dim,)), ((), ())), preferred_element_type=F32
    )


def sigmoid(v):
    return 0.5 * jnp.tanh(0.5 * v) + 0.5


def whole(shape):
    zeros = (0,) * len(shape)
    return pl.BlockSpec(shape, lambda *_: zeros, pipeline_mode=pl.Buffered(1))


def settings(dims, mib):
    return pltpu.CompilerParams(
        dimension_semantics=("arbitrary",) * dims, vmem_limit_bytes=mib << 20
    )


def shape_of(shape, dtype):
    return jax.ShapeDtypeStruct(shape, dtype)


def cost(large):
    size = 1 << 42 if large else 1 << 10
    return pl.CostEstimate(flops=size, bytes_accessed=size >> 12, transcendentals=0)


def pack_kernel(info, o_in, g_in, u_in, d_in, *refs):
    out_ref, ffn_ref, first_ref, second_ref, third_ref, o_ref, g_ref, u_ref, d_ref, sems = refs
    ctx = info[2]
    pairs = ((o_in, o_ref), (g_in, g_ref), (u_in, u_ref), (d_in, d_ref))
    copies = [pltpu.make_async_copy(a, b, sems.at[i]) for i, (a, b) in enumerate(pairs)]
    for copy in copies:
        copy.start()
    for copy in copies:
        copy.wait()
    o_t = o_ref[...].astype(F32).T.astype(BF16)
    out_ref[...] = o_t
    third = g_ref.shape[1] // 3
    first_ref[:, 3 * third :] = o_t
    for j, chunk in enumerate((first_ref, second_ref, third_ref)):
        at = pl.multiple_of(jnp.where(ctx == 0, j, 2 - j) * third, third)
        parts = [
            g_ref[:, pl.ds(at, third)],
            u_ref[:, pl.ds(at, third)],
            d_ref[pl.ds(at, third), :].astype(F32).T.astype(BF16),
        ]
        for i, part in enumerate(parts):
            chunk[:, i * third : (i + 1) * third] = part
            ffn_ref[:, (3 * j + i) * third : (3 * j + i + 1) * third] = part


def pack(info, o, g, u, d):
    rows, units = g.shape
    feats = o.shape[0]
    widths = (feats, 3 * units, units + feats, units, units)
    return pl.pallas_call(
        pack_kernel,
        in_specs=[SMEM] + [ANY] * 4,
        out_specs=[pl.BlockSpec(memory_space=pltpu.VMEM)] * 5,
        out_shape=[shape_of((rows, n), BF16) for n in widths],
        scratch_shapes=[pltpu.VMEM(a.shape, BF16) for a in (o, g, u, d)]
        + [pltpu.SemaphoreType.DMA((4,))],
        compiler_params=pltpu.CompilerParams(vmem_limit_bytes=24 << 20),
        cost_estimate=cost(False),
        name="pack",
    )(info, o, g, u, d)


def join_kernel(q_ref, k_ref, v_ref, out_ref):
    at = 0
    for ref in (q_ref, k_ref, v_ref):
        out_ref[:, at : at + ref.shape[1]] = ref[...]
        at += ref.shape[1]


def join(q, k, v):
    return pl.pallas_call(
        join_kernel,
        out_shape=shape_of((q.shape[0], q.shape[1] + k.shape[1] + v.shape[1]), BF16),
        compiler_params=pltpu.CompilerParams(vmem_limit_bytes=8 << 20),
        cost_estimate=cost(False),
        name="join",
    )(q, k, v)


def norm_one_kernel(info, tok_ref, gain_ref, x_ref, nt_ref, x32):
    quarter = x_ref.shape[1] // 4
    for p, mask in enumerate(MASKS):
        at = pl.multiple_of(jnp.bitwise_xor(info[1], mask) * quarter, quarter)
        part = tok_ref[0, :, pl.ds(at, quarter)]
        x_ref[:, p * quarter : (p + 1) * quarter] = part
        x32[:, p * quarter : (p + 1) * quarter] = part.astype(F32)
    x = x32[...]
    rho = lax.rsqrt(jnp.mean(x * x, axis=-1, keepdims=True) + EPS)
    nt_ref[...] = (x * rho * gain_ref[...]).T.astype(BF16)


def norm_one(info, tokens, gain, tile):
    _, tok, width = tokens.shape
    return pl.pallas_call(
        norm_one_kernel,
        grid_spec=pltpu.PrefetchScalarGridSpec(
            num_scalar_prefetch=1,
            grid=(tok // tile,),
            in_specs=[
                pl.BlockSpec((1, tile, width), lambda i, info: (info[0], i, 0)),
                pl.BlockSpec((1, width), lambda i, info: (0, 0)),
            ],
            out_specs=[
                pl.BlockSpec((tile, width), lambda i, info: (i, 0)),
                pl.BlockSpec((width, tile), lambda i, info: (0, i)),
            ],
            scratch_shapes=[pltpu.VMEM((tile, width), F32)],
        ),
        out_shape=[shape_of((tok, width), BF16), shape_of((width, tok), BF16)],
        compiler_params=settings(1, 24),
        cost_estimate=cost(False),
        name="norm_one",
    )(info, tokens, gain)


def proj_kernel(heads, block, plan, count, info, *refs):
    nt_ref, cos_ref, sin_ref, qg_ref, kg_ref, rot_ref, raw_ref, w_ref, sem = refs[count:]
    rows = w_ref.shape[0] // 4

    @pl.when(pl.program_id(0) == 0)
    def _():
        for k in range(4):

            @pl.when(block(info) == k)
            def _():
                for p, (piece, row) in enumerate(plan[k]):
                    src = refs[piece].at[pl.ds(row, rows)]
                    pltpu.make_async_copy(src, w_ref.at[pl.ds(p * rows, rows)], sem).start()

        pltpu.make_async_copy(w_ref, w_ref, sem).wait()

    hd = qg_ref.shape[0]
    half = hd // 2
    raw = dot(w_ref[...], nt_ref[...], 0, 0)
    cos_part, sin_part = cos_ref[...], sin_ref[...]
    heads_q, heads_k = heads
    raw_ref[...] = raw.astype(BF16)
    for h in range(heads_q + heads_k):
        v = raw[h * hd : (h + 1) * hd]
        rho = lax.rsqrt(jnp.mean(v * v, axis=0, keepdims=True) + EPS)
        v = v * rho * (qg_ref[...] if h < heads_q else kg_ref[...])
        a, b = v[:half], v[half:]
        rot_ref[h * hd : h * hd + half, :] = (a * cos_part - b * sin_part).astype(BF16)
        rot_ref[h * hd + half : (h + 1) * hd, :] = (b * cos_part + a * sin_part).astype(BF16)
    at = (heads_q + heads_k) * hd
    rot_ref[at:, :] = raw[at:].astype(BF16)


def project(info, weights, normed_t, cos_part, sin_part, gain_q, gain_k, heads, block):
    plan, pieces = weights
    width, tok = normed_t.shape
    cols = pieces[0].shape[1]
    tile = min(512, tok)
    const = lambda a: pl.BlockSpec(a.shape, lambda i, info: (0, 0))
    tab = lambda a: pl.BlockSpec((a.shape[0], tile), lambda i, info: (0, i))
    return pl.pallas_call(
        functools.partial(proj_kernel, heads, block, plan, len(pieces)),
        grid_spec=pltpu.PrefetchScalarGridSpec(
            num_scalar_prefetch=1,
            grid=(tok // tile,),
            in_specs=[ANY] * len(pieces)
            + [tab(normed_t), tab(cos_part), tab(sin_part), const(gain_q), const(gain_k)],
            out_specs=[pl.BlockSpec((cols, tile), lambda i, info: (0, i))] * 2,
            scratch_shapes=[pltpu.VMEM((width, cols), BF16), pltpu.SemaphoreType.DMA],
        ),
        out_shape=[shape_of((cols, tok), BF16), shape_of((cols, tok), BF16)],
        compiler_params=settings(1, 24),
        cost_estimate=cost(False),
        name="project",
    )(info, *pieces, normed_t, cos_part, sin_part, gain_q, gain_k)


def head_back_kernel(
    heads, info, dm_ref, dt_ref, rm_ref, rt_ref, cos_ref, sin_ref, qg_ref, kg_ref, out_ref, gg_ref
):
    step, part = pl.program_id(0), pl.program_id(1)
    hd = qg_ref.shape[0]
    half = hd // 2
    heads_q, heads_k = heads
    cos_part, sin_part = cos_ref[...], sin_ref[...]
    tile = cos_part.shape[1]

    @pl.when((step == 0) & (part == 0))
    def _():
        gg_ref[...] = jnp.zeros_like(gg_ref)

    def work(d_ref, r_ref):
        gain_q = jnp.zeros((hd, 1), F32)
        gain_k = jnp.zeros((hd, 1), F32)
        done = []
        for h in range(heads_q + heads_k):
            is_q = h < heads_q
            g = d_ref[h * hd : (h + 1) * hd, :].astype(F32)
            raw = r_ref[h * hd : (h + 1) * hd, :].astype(F32)
            a, b = g[:half], g[half:]
            turned = jnp.concatenate(
                [a * cos_part + b * sin_part, b * cos_part - a * sin_part], axis=0
            )
            rho = lax.rsqrt(jnp.mean(raw * raw, axis=0, keepdims=True) + EPS)
            unit = raw * rho
            prod = turned * unit
            scaled = turned * (qg_ref[...] if is_q else kg_ref[...])
            mean = jnp.mean(scaled * unit, axis=0, keepdims=True)
            done.append(rho * (scaled - unit * mean))
            total = jnp.sum(prod, axis=1, keepdims=True)
            if is_q:
                gain_q = gain_q + total
            else:
                gain_k = gain_k + total
        done.append(d_ref[(heads_q + heads_k) * hd :, :].astype(F32))
        out_ref[0] = jnp.concatenate(done, axis=0).T.astype(BF16)
        lane = lax.broadcasted_iota(jnp.int32, gg_ref.shape, 1)
        gg_ref[...] += jnp.where(lane == 0, gain_q, jnp.where(lane == 1, gain_k, 0.0))

    @pl.when(step == 0)
    def _():
        work(dm_ref, rm_ref)

    @pl.when(step == 1)
    def _():
        work(dt_ref, rt_ref)


def head_back(info, grad_mine, grad_theirs, raw_mine, raw_theirs, cos_part, sin_part, gq, gk, heads):
    cols, tok = grad_mine.shape
    tile = min(512, tok)
    mine = pl.BlockSpec((cols, tile), lambda s, i, info: (0, jnp.where(s == 0, i, tok // tile - 1)))
    theirs = pl.BlockSpec((cols, tile), lambda s, i, info: (0, jnp.where(s == 0, 0, i)))
    tab = lambda a: pl.BlockSpec((a.shape[0], tile), lambda s, i, info: (0, i))
    const = lambda a: pl.BlockSpec(a.shape, lambda s, i, info: (0, 0))
    return pl.pallas_call(
        functools.partial(head_back_kernel, heads),
        grid_spec=pltpu.PrefetchScalarGridSpec(
            num_scalar_prefetch=1,
            grid=(2, tok // tile),
            in_specs=[
                mine,
                theirs,
                mine,
                theirs,
                tab(cos_part),
                tab(sin_part),
                const(gq),
                const(gk),
            ],
            out_specs=[
                pl.BlockSpec(
                    (1, tile, cols), lambda s, i, info: (jnp.bitwise_xor(info[2], s), i, 0)
                ),
                pl.BlockSpec((gq.shape[0], 128), lambda s, i, info: (0, 0)),
            ],
        ),
        out_shape=[shape_of((2, tok, cols), BF16), shape_of((gq.shape[0], 128), F32)],
        compiler_params=settings(2, 24),
        cost_estimate=cost(False),
        name="head_back",
    )(info, grad_mine, grad_theirs, raw_mine, raw_theirs, cos_part, sin_part, gq, gk)


def load_rows(info, mine_ref, got_ref, rows, sems):
    tok = mine_ref.shape[1]
    ctx = info[2]
    here = pl.multiple_of(ctx * tok, tok)
    there = pl.multiple_of((1 - ctx) * tok, tok)
    one = pltpu.make_async_copy(mine_ref, rows.at[:, pl.ds(here, tok)], sems.at[0])
    two = pltpu.make_async_copy(got_ref, rows.at[:, pl.ds(there, tok)], sems.at[1])
    one.start()
    two.start()
    one.wait()
    two.wait()


def keys_with_bias(keys, length):
    hd, slots = keys.shape
    pos = lax.broadcasted_iota(jnp.int32, (hd, slots), 1)
    row = lax.broadcasted_iota(jnp.int32, (hd, slots), 0)
    bias = jnp.where((row == 0) & (pos >= length), NEGATIVE, 0.0)
    return jnp.concatenate([keys.astype(F32), bias], axis=0).T.astype(BF16)


def query_with_one(pair):
    one_row = jnp.where(lax.broadcasted_iota(jnp.int32, pair.shape, 0) == 0, 1.0, 0.0)
    return jnp.concatenate([pair, one_row.astype(BF16)], axis=0)


def causal(scores, width):
    key_pos = lax.broadcasted_iota(jnp.int32, (width, width), 0)
    query_pos = lax.broadcasted_iota(jnp.int32, (width, width), 1)
    allowed = key_pos <= query_pos
    return jnp.where(jnp.concatenate([allowed, allowed], axis=1), scores, NEGATIVE)


def attn_fwd_kernel(
    width, hd, info, mine_ref, got_ref, keep_ref, send_ref, lse_ref, rows, key_rows, sems
):
    head, block = pl.program_id(0), pl.program_id(1)
    heads_k = pl.num_programs(0)
    scale = hd**-0.5 * LOG2E
    length = info[3]
    key_at = pl.multiple_of(heads_k * 2 * hd + head * hd, hd)
    value_at = pl.multiple_of(heads_k * 3 * hd + head * hd, hd)
    query_at = pl.multiple_of(head * 2 * hd, 2 * hd)

    @pl.when((head == 0) & (block == 0))
    def _():
        load_rows(info, mine_ref, got_ref, rows, sems)

    @pl.when(block == 0)
    def _():
        key_rows[...] = keys_with_bias(rows[pl.ds(key_at, hd), :], length)

    start = pl.multiple_of(block * width, width)
    both = rows[pl.ds(query_at, 2 * hd), pl.ds(start, width)]
    query = query_with_one(jnp.concatenate([both[:hd], both[hd:]], axis=1))

    def tile(at, carried, diagonal):
        out, total = carried
        scores = dot(key_rows[pl.ds(at, width), :], query, 1, 0)
        if diagonal:
            scores = causal(scores, width)
        probs = jnp.exp2(scores * scale)
        total = total + jnp.sum(probs, axis=0, keepdims=True)
        out = out + dot(rows[pl.ds(value_at, hd), pl.ds(at, width)], probs.astype(BF16), 1, 0)
        return out, total

    carried = (jnp.zeros((hd, 2 * width), F32), jnp.zeros((1, 2 * width), F32))
    full = jnp.minimum(block, lax.div(length + width - 1, width))
    carried = lax.fori_loop(
        0, full, lambda j, c: tile(pl.multiple_of(j * width, width), c, False), carried
    )
    out, total = tile(start, carried, True)
    out = out * (1.0 / total)
    out = jnp.concatenate([out[:, :width], out[:, width:]], axis=0).T.astype(BF16)
    here = block // 2 == info[2]

    @pl.when(here)
    def _():
        keep_ref[...] = out

    @pl.when(jnp.logical_not(here))
    def _():
        send_ref[...] = out

    log_total = jnp.log2(total)
    lse_ref[0, 0:1, :] = log_total[:, :width]
    lse_ref[0, 1:2, :] = log_total[:, width:]


def keep_block(i, info):
    return jnp.clip(i - 2 * info[2], 0, 1)


def send_block(i, info):
    return jnp.clip(i - 2 * (1 - info[2]), 0, 1)


def attn_fwd(info, mine, got, hd):
    cols, tok = mine.shape
    heads_k = cols // (4 * hd)
    width = tok // 2
    return pl.pallas_call(
        functools.partial(attn_fwd_kernel, width, hd),
        grid_spec=pltpu.PrefetchScalarGridSpec(
            num_scalar_prefetch=1,
            grid=(heads_k, 4),
            in_specs=[ANY, ANY],
            out_specs=[
                pl.BlockSpec((width, 2 * hd), lambda h, i, info: (keep_block(i, info), h)),
                pl.BlockSpec((width, 2 * hd), lambda h, i, info: (send_block(i, info), h)),
                pl.BlockSpec((1, 2, width), lambda h, i, info: (h, 0, i)),
            ],
            scratch_shapes=[
                pltpu.VMEM((cols, 2 * tok), BF16),
                pltpu.VMEM((2 * tok, 2 * hd), BF16),
                pltpu.SemaphoreType.DMA((2,)),
            ],
        ),
        out_shape=[
            shape_of((tok, heads_k * 2 * hd), BF16),
            shape_of((tok, heads_k * 2 * hd), BF16),
            shape_of((heads_k, 2, 2 * tok), F32),
        ],
        compiler_params=settings(2, 60),
        cost_estimate=cost(True),
        name="attn_fwd",
    )(info, mine, got)


def attn_bwd_kernel(
    width,
    hd,
    info,
    mine_ref,
    got_ref,
    ok_ref,
    os_ref,
    gk_ref,
    gs_ref,
    lse_ref,
    keep_ref,
    send_ref,
    rows,
    key_rows,
    value_rows,
    key_sum,
    value_sum,
    sems,
):
    head, block = pl.program_id(0), pl.program_id(1)
    heads_k = pl.num_programs(0)
    scale = hd**-0.5
    length = info[3]
    ctx = info[2]
    tok = keep_ref.shape[1]
    key_at = pl.multiple_of(heads_k * 2 * hd + head * hd, hd)
    value_at = pl.multiple_of(heads_k * 3 * hd + head * hd, hd)
    query_at = pl.multiple_of(head * 2 * hd, 2 * hd)

    @pl.when((head == 0) & (block == 0))
    def _():
        load_rows(info, mine_ref, got_ref, rows, sems)

    @pl.when(block == 0)
    def _():
        key_rows[...] = keys_with_bias(rows[pl.ds(key_at, hd), :], length)
        value_rows[...] = rows[pl.ds(value_at, hd), :].astype(F32).T.astype(BF16)
        key_sum[...] = jnp.zeros_like(key_sum)
        value_sum[...] = jnp.zeros_like(value_sum)

    start = pl.multiple_of(block * width, width)
    here = block // 2 == ctx

    def store_query(value):
        at = pl.ds(pl.multiple_of((block % 2) * width, width), width)

        @pl.when(here)
        def _():
            keep_ref[pl.ds(query_at, 2 * hd), at] = value

        @pl.when(jnp.logical_not(here))
        def _():
            send_ref[pl.ds(query_at, 2 * hd), at] = value

    @pl.when(block * width < length)
    def _():
        both = rows[pl.ds(query_at, 2 * hd), pl.ds(start, width)]
        pair = jnp.concatenate([both[:hd], both[hd:]], axis=1)
        query = query_with_one(pair)
        query_rows = pair.astype(F32).T.astype(BF16)
        grad_wide = jnp.where(here, gk_ref[...].astype(F32), gs_ref[...].astype(F32))
        out_wide = jnp.where(here, ok_ref[...].astype(F32), os_ref[...].astype(F32))
        grad_rows = jnp.concatenate([grad_wide[:, :hd], grad_wide[:, hd:]], axis=0).astype(BF16)
        grad_t = grad_wide.T
        prod = (grad_wide * out_wide).T
        grad = jnp.concatenate([grad_t[:hd], grad_t[hd:]], axis=1).astype(BF16)
        delta = jnp.concatenate(
            [
                jnp.sum(prod[:hd], axis=0, keepdims=True),
                jnp.sum(prod[hd:], axis=0, keepdims=True),
            ],
            axis=1,
        )
        lse = jnp.concatenate([lse_ref[0, 0:1, :], lse_ref[0, 1:2, :]], axis=1)

        def tile(at, query_sum, diagonal):
            scores = dot(key_rows[pl.ds(at, width), :], query, 1, 0)
            if diagonal:
                scores = causal(scores, width)
            probs = jnp.exp2(scores * (scale * LOG2E) - lse)
            grad_probs = dot(value_rows[pl.ds(at, width), :], grad, 1, 0)
            grad_scores = (probs * (grad_probs - delta)).astype(BF16)
            value_sum[pl.ds(at, width), :] += dot(probs.astype(BF16), grad_rows, 1, 0)
            key_sum[pl.ds(at, width), :] += dot(grad_scores, query_rows, 1, 0)
            return query_sum + dot(rows[pl.ds(key_at, hd), pl.ds(at, width)], grad_scores, 1, 0)

        query_sum = lax.fori_loop(
            0,
            block,
            lambda j, s: tile(pl.multiple_of(j * width, width), s, False),
            jnp.zeros((hd, 2 * width), F32),
        )
        query_sum = tile(start, query_sum, True) * scale
        store_query(
            jnp.concatenate([query_sum[:, :width], query_sum[:, width:]], axis=0).astype(BF16)
        )

    @pl.when(block * width >= length)
    def _():
        store_query(jnp.zeros((2 * hd, width), BF16))

    @pl.when(block == 3)
    def _():
        for at, total in ((key_at, key_sum[...] * scale), (value_at, value_sum[...])):
            total = total.T.astype(BF16)
            left, right = total[:, :tok], total[:, tok:]

            @pl.when(ctx == 0)
            def _():
                keep_ref[pl.ds(at, hd), :] = left
                send_ref[pl.ds(at, hd), :] = right

            @pl.when(ctx == 1)
            def _():
                keep_ref[pl.ds(at, hd), :] = right
                send_ref[pl.ds(at, hd), :] = left


def attn_bwd(info, mine, got, out_keep, out_send, grad_keep, grad_send, lse, hd):
    cols, tok = mine.shape
    heads_k = cols // (4 * hd)
    width = tok // 2
    keep = pl.BlockSpec((width, 2 * hd), lambda h, i, info: (keep_block(i, info), h))
    send = pl.BlockSpec((width, 2 * hd), lambda h, i, info: (send_block(i, info), h))
    full = pl.BlockSpec((cols, tok), lambda h, i, info: (0, 0))
    return pl.pallas_call(
        functools.partial(attn_bwd_kernel, width, hd),
        grid_spec=pltpu.PrefetchScalarGridSpec(
            num_scalar_prefetch=1,
            grid=(heads_k, 4),
            in_specs=[
                ANY,
                ANY,
                keep,
                send,
                keep,
                send,
                pl.BlockSpec((1, 2, width), lambda h, i, info: (h, 0, i)),
            ],
            out_specs=[full, full],
            scratch_shapes=[
                pltpu.VMEM((cols, 2 * tok), BF16),
                pltpu.VMEM((2 * tok, 2 * hd), BF16),
                pltpu.VMEM((2 * tok, hd), BF16),
                pltpu.VMEM((2 * tok, hd), F32),
                pltpu.VMEM((2 * tok, hd), F32),
                pltpu.SemaphoreType.DMA((2,)),
            ],
        ),
        out_shape=[shape_of((cols, tok), BF16), shape_of((cols, tok), BF16)],
        compiler_params=settings(2, 60),
        cost_estimate=cost(True),
        name="attn_bwd",
    )(info, mine, got, out_keep, out_send, grad_keep, grad_send, lse)


def load_blocks(plan, pieces, target, sem):
    rows = target.shape[1] // 4

    @pl.when(pl.program_id(0) == 0)
    def _():
        for k, places in enumerate(plan):
            for p, (piece, row) in enumerate(places):
                src = pieces[piece].at[pl.ds(row, rows)]
                pltpu.make_async_copy(src, target.at[k, pl.ds(p * rows, rows)], sem).start()
        pltpu.make_async_copy(target, target, sem).wait()


def out_proj_kernel(plan, count, info, *refs):
    x_ref, a0, a1, b0, b1, gain_ref, r_ref, n_ref, nt_ref, att_ref, w_ref, sem = refs[count:]
    load_blocks(plan, refs, w_ref, sem)
    ctx = info[2]
    total = x_ref[...].astype(F32)
    for j, ref, side in ((0, a0, ctx), (1, a1, ctx), (0, b0, 1 - ctx), (1, b1, 1 - ctx)):
        block = 2 * side + j
        part = ref[...]
        att_ref[block] = part
        total = total + dot(part, w_ref[block], 1, 1)
    rho = lax.rsqrt(jnp.mean(total * total, axis=-1, keepdims=True) + EPS)
    normed = total * rho * gain_ref[...]
    r_ref[...] = total
    n_ref[...] = normed.astype(BF16)
    nt_ref[...] = normed.T.astype(BF16)


def out_proj(info, x, mine, theirs, weights, gain, tile):
    plan, pieces = weights
    tok, width = x.shape
    feats = pieces[0].shape[1]
    rows_of = lambda n: pl.BlockSpec((tile, n), lambda i, info: (i, 0))
    return pl.pallas_call(
        functools.partial(out_proj_kernel, plan, len(pieces)),
        grid_spec=pltpu.PrefetchScalarGridSpec(
            num_scalar_prefetch=1,
            grid=(tok // tile,),
            in_specs=[ANY] * len(pieces)
            + [rows_of(width)]
            + [rows_of(feats)] * 4
            + [pl.BlockSpec((1, width), lambda i, info: (0, 0))],
            out_specs=[
                rows_of(width),
                rows_of(width),
                pl.BlockSpec((width, tile), lambda i, info: (0, i)),
                pl.BlockSpec((4, tile, feats), lambda i, info: (0, i, 0)),
            ],
            scratch_shapes=[pltpu.VMEM((4, width, feats), BF16), pltpu.SemaphoreType.DMA],
        ),
        out_shape=[
            shape_of((tok, width), F32),
            shape_of((tok, width), BF16),
            shape_of((width, tok), BF16),
            shape_of((4, tok, feats), BF16),
        ],
        compiler_params=settings(1, 32),
        cost_estimate=cost(True),
        name="out_proj",
    )(info, *pieces, x, *mine, *theirs, gain)


def norm_two_back_kernel(plan, count, info, *refs):
    g_ref, r_ref, gr_ref, gain_ref, gres_ref, gat_ref, a0, a1, b0, b1, gg_ref, w_ref, sem = refs[count:]
    load_blocks(plan, refs, w_ref, sem)
    ctx = info[2]
    grad, resid = g_ref[...], r_ref[...]
    rho = lax.rsqrt(jnp.mean(resid * resid, axis=-1, keepdims=True) + EPS)
    unit = resid * rho
    scaled = grad * gain_ref[...]
    back = rho * (scaled - unit * jnp.mean(scaled * unit, axis=-1, keepdims=True))
    total = gr_ref[...] + back
    gres_ref[...] = total
    low = total.astype(BF16)
    gat_ref[...] = total.T.astype(BF16)

    @pl.when(pl.program_id(0) == 0)
    def _():
        gg_ref[...] = jnp.zeros_like(gg_ref)

    gg_ref[...] += jnp.sum(grad * unit, axis=0, keepdims=True)
    for j, ref, side in ((0, a0, ctx), (1, a1, ctx), (0, b0, 1 - ctx), (1, b1, 1 - ctx)):
        ref[...] = dot(low, w_ref[2 * side + j], 1, 0).astype(BF16)


def norm_two_back(info, grad, resid, grad_result, gain, weights, tile):
    plan, pieces = weights
    tok, width = grad.shape
    feats = pieces[0].shape[1]
    rows_of = lambda n: pl.BlockSpec((tile, n), lambda i, info: (i, 0))
    row = pl.BlockSpec((1, width), lambda i, info: (0, 0))
    return pl.pallas_call(
        functools.partial(norm_two_back_kernel, plan, len(pieces)),
        grid_spec=pltpu.PrefetchScalarGridSpec(
            num_scalar_prefetch=1,
            grid=(tok // tile,),
            in_specs=[ANY] * len(pieces) + [rows_of(width)] * 3 + [row],
            out_specs=[rows_of(width), pl.BlockSpec((width, tile), lambda i, info: (0, i))]
            + [rows_of(feats)] * 4
            + [row],
            scratch_shapes=[pltpu.VMEM((4, width, feats), BF16), pltpu.SemaphoreType.DMA],
        ),
        out_shape=[shape_of((tok, width), F32), shape_of((width, tok), BF16)]
        + [shape_of((tok, feats), BF16)] * 4
        + [shape_of((1, width), F32)],
        compiler_params=settings(1, 32),
        cost_estimate=cost(True),
        name="norm_two_back",
    )(info, *pieces, grad, resid, grad_result, gain)


def norm_one_back_kernel(plan, count, info, *refs):
    p0, p1, x_ref, gres_ref, gain_ref, *out_refs, gg_ref, w_ref, sem = refs[count:]
    load_blocks(plan, refs, w_ref, sem)
    quarter = x_ref.shape[1] // 4
    grad = dot(p0[0], w_ref[0], 1, 1)
    grad = grad + dot(p1[0], w_ref[1], 1, 1)
    grad = grad + dot(p0[1], w_ref[2], 1, 1)
    grad = grad + dot(p1[1], w_ref[3], 1, 1)
    x = x_ref[...].astype(F32)
    rho = lax.rsqrt(jnp.mean(x * x, axis=-1, keepdims=True) + EPS)
    unit = x * rho
    scaled = grad * gain_ref[...]
    back = rho * (scaled - unit * jnp.mean(scaled * unit, axis=-1, keepdims=True))
    total = (gres_ref[...] + back).astype(BF16)
    for p, mask in enumerate(MASKS):
        at = pl.multiple_of(jnp.bitwise_xor(info[1], mask) * quarter, quarter)
        part = total[:, p * quarter : (p + 1) * quarter]

        for i, out_ref in enumerate(out_refs):

            @pl.when(pl.program_id(0) == i)
            def _():
                out_ref[:, pl.ds(at, quarter)] = part

    @pl.when(pl.program_id(0) == 0)
    def _():
        gg_ref[...] = jnp.zeros_like(gg_ref)

    gg_ref[...] += jnp.sum(grad * unit, axis=0, keepdims=True)


def norm_one_back(info, pairs, weights, x, grad_resid, gain, tile):
    plan, pieces = weights
    tok, width = x.shape
    cols = pieces[0].shape[1]
    rows_of = lambda n: pl.BlockSpec((tile, n), lambda i, info: (i, 0))
    pair = pl.BlockSpec((2, tile, cols), lambda i, info: (0, i, 0))
    row = pl.BlockSpec((1, width), lambda i, info: (0, 0))
    return pl.pallas_call(
        functools.partial(norm_one_back_kernel, plan, len(pieces)),
        grid_spec=pltpu.PrefetchScalarGridSpec(
            num_scalar_prefetch=1,
            grid=(tok // tile,),
            in_specs=[ANY] * len(pieces) + [pair, pair, rows_of(width), rows_of(width), row],
            out_specs=[pl.BlockSpec((tile, width), lambda i, info: (0, 0))] * 4 + [row],
            scratch_shapes=[pltpu.VMEM((4, width, cols), BF16), pltpu.SemaphoreType.DMA],
        ),
        out_shape=[shape_of((tile, width), BF16)] * 4 + [shape_of((1, width), F32)],
        compiler_params=settings(1, 32),
        cost_estimate=cost(True),
        name="norm_one_back",
    )(info, *pieces, *pairs, x, grad_resid, gain)


def weight_copies(plan, pieces, gate_up, down, gate_up_sem, down_sem):
    third = down.shape[1] // 3
    rows = down.shape[0] // 4
    wide, thin = [], []
    for p, chunks in enumerate(plan):
        block = pl.ds(p * rows, rows)
        for j, (piece, row, at) in enumerate(chunks):
            src = pieces[piece].at[pl.ds(row, rows)]
            wide.append(
                pltpu.make_async_copy(
                    src.at[:, pl.ds(at, 2 * third)],
                    gate_up.at[block, pl.ds(j * 2 * third, 2 * third)],
                    gate_up_sem,
                )
            )
            thin.append(
                pltpu.make_async_copy(
                    src.at[:, pl.ds(at + 2 * third, third)],
                    down.at[block, pl.ds(j * third, third)],
                    down_sem,
                )
            )
    return wide, thin


def split_act(act):
    third = act.shape[1] // 6
    part = lambda j: act[:, j * third : (j + 1) * third]
    return [(part(0), part(1)), (part(2), part(3)), (part(4), part(5))]


def ffn_fwd_kernel(tile, plans, last, info, scale, x_ref, in_ref, *rest):
    if last:
        teach_ref, rest = rest[0], rest[1:]
    pieces = []
    for plan in plans:
        count = 1 + max(place[0] for chunks in plan for place in chunks)
        pieces.append(rest[:count])
        rest = rest[count:]
    act_ref, hid_ref = rest[:2]
    if last:
        outa_ref, outb_ref, gres_ref, low_ref, lowt_ref, sq_ref = rest[2:8]
        gate_up, down, total, sems = rest[8:]
    else:
        sum_ref, gate_up, down, total, sems = rest[2:]
    step, part = pl.program_id(0), pl.program_id(1)
    final = len(plans) - 1
    width = x_ref.shape[1]
    quarter = width // 4
    third = down.shape[2] // 3

    def copies(s):
        return weight_copies(
            plans[s], pieces[s], gate_up.at[s], down.at[s], sems.at[s, 0], sems.at[s, 1]
        )

    @pl.when((step == 0) & (part == 0))
    def _():
        for s in range(len(plans)):
            wide, thin = copies(s)
            for copy in wide + thin:
                copy.start()

    for s in range(len(plans)):

        @pl.when((step == s) & (part == 0))
        def _():
            pltpu.make_async_copy(gate_up.at[s], gate_up.at[s], sems.at[s, 0]).wait()
            pltpu.make_async_copy(down.at[s], down.at[s], sems.at[s, 1]).wait()

    rows = pl.ds(pl.multiple_of(part * tile, tile), tile)
    act = dot(x_ref[rows, :], gate_up[step], 1, 0)
    for j, (gate, upper) in enumerate(split_act(act)):
        hid_ref[0, :, j * third : (j + 1) * third] = (gate * sigmoid(gate) * upper).astype(BF16)
    act_ref[0] = act.astype(BF16)
    grown = dot(hid_ref[0], down[step], 1, 1)

    @pl.when(step == 0)
    def _():
        total[rows, :] = in_ref[...] + grown

    @pl.when(step > 0)
    def _():
        total[rows, :] += grown

    @pl.when(step == final)
    def _():
        result = total[rows, :]
        if not last:
            sum_ref[...] = result
            return
        tok = x_ref.shape[0]
        slot = info[2] * tok + part * tile + lax.broadcasted_iota(jnp.int32, (tile, 1), 0)
        valid = jnp.where(slot < info[3], 1.0, 0.0)
        square = jnp.zeros((tile, quarter), F32)
        for p, mask in enumerate(MASKS):
            at = pl.multiple_of(jnp.bitwise_xor(info[1], mask) * quarter, quarter)
            cols = slice(p * quarter, (p + 1) * quarter)
            value = result[:, cols]
            low = value.astype(BF16)

            @pl.when(part < pl.num_programs(1) // 2)
            def _():
                outa_ref[:, pl.ds(at, quarter)] = low

            @pl.when(part >= pl.num_programs(1) // 2)
            def _():
                outb_ref[:, pl.ds(at, quarter)] = low

            error = valid * (value - teach_ref[0, :, pl.ds(at, quarter)].astype(F32))
            square = square + error * error
            grad = error * scale[0]
            gres_ref[:, cols] = grad
            low_ref[:, cols] = grad.astype(BF16)
            lowt_ref[cols, :] = grad.T.astype(BF16)

        @pl.when(part == 0)
        def _():
            sq_ref[...] = jnp.zeros_like(sq_ref)

        sq_ref[...] += jnp.sum(square, axis=0, keepdims=True)


def ffn_fwd(info, scale, x, total, teacher, weights, units, tile):
    tok, width = x.shape
    pieces = [piece for _, group in weights for piece in group]
    count = len(weights)
    last = teacher is not None
    entry = lambda s, i: jnp.where(s == 0, i, tok // tile - 1)
    leave = lambda s, i: jnp.where(s == count - 1, i, 0)
    tiles = lambda n: pl.BlockSpec((tile, n), lambda s, i, info: (leave(s, i), 0))
    slab = lambda n: pl.BlockSpec((1, tile, n), lambda s, i, info: (s, i, 0))
    in_specs = [
        SMEM,
        whole((tok, width)),
        pl.BlockSpec((tile, width), lambda s, i, info: (entry(s, i), 0)),
    ]
    out_specs = [slab(2 * units), slab(units)]
    out_shape = [shape_of((count, tok, 2 * units), BF16), shape_of((count, tok, units), BF16)]
    if last:
        in_specs.append(
            pl.BlockSpec((1, tile, width), lambda s, i, info: (info[0], leave(s, i), 0))
        )
        half = tok // tile // 2
        out_specs += [
            pl.BlockSpec(
                (tile, width), lambda s, i, info: (jnp.minimum(leave(s, i), half - 1), 0)
            ),
            pl.BlockSpec(
                (tile, width), lambda s, i, info: (jnp.maximum(leave(s, i) - half, 0), 0)
            ),
            tiles(width),
            tiles(width),
            pl.BlockSpec((width, tile), lambda s, i, info: (0, leave(s, i))),
            pl.BlockSpec((1, width // 4), lambda s, i, info: (0, 0)),
        ]
        out_shape += [
            shape_of((tok // 2, width), BF16),
            shape_of((tok // 2, width), BF16),
            shape_of((tok, width), F32),
            shape_of((tok, width), BF16),
            shape_of((width, tok), BF16),
            shape_of((1, width // 4), F32),
        ]
    else:
        out_specs.append(tiles(width))
        out_shape.append(shape_of((tok, width), F32))
    return pl.pallas_call(
        functools.partial(ffn_fwd_kernel, tile, [plan for plan, _ in weights], last),
        grid_spec=pltpu.PrefetchScalarGridSpec(
            num_scalar_prefetch=1,
            grid=(count, tok // tile),
            in_specs=in_specs + [ANY] * len(pieces),
            out_specs=out_specs,
            scratch_shapes=[
                pltpu.VMEM((count, width, 2 * units), BF16),
                pltpu.VMEM((count, width, units), BF16),
                pltpu.VMEM((tok, width), F32),
                pltpu.SemaphoreType.DMA((count, 2)),
            ],
        ),
        out_shape=out_shape,
        compiler_params=settings(2, 60),
        cost_estimate=cost(True),
        name="ffn_fwd",
    )(info, scale, x, total, *([teacher] if last else []), *pieces)


def ffn_bwd_kernel(steps, plan, first, low_ref, act_ref, hid_ref, xt_ref, lowt_ref, *rest):
    count = 1 + max(place[0] for chunks in plan for place in chunks)
    pieces, rest = rest[:count], rest[count:]
    if not first:
        in_ref, rest = rest[0], rest[1:]
    out_ref, keep_ref, send_ref, gate_up, down, dact_all, hid_all, sems = rest
    step = pl.program_id(0)
    units = down.shape[1]
    third = units // 3
    tile = low_ref.shape[0]

    @pl.when(step == 0)
    def _():
        wide, thin = weight_copies(plan, pieces, gate_up, down, sems.at[0], sems.at[1])
        for copy in thin + wide:
            copy.start()
        pltpu.make_async_copy(down, down, sems.at[1]).wait()

    @pl.when(step < steps)
    def _():
        rows = pl.ds(pl.multiple_of(step * tile, tile), tile)
        grad_hidden = dot(low_ref[...], down[...], 1, 0)
        for j, (gate, upper) in enumerate(split_act(act_ref[0])):
            grad = grad_hidden[:, j * third : (j + 1) * third]
            gate, upper = gate.astype(F32), upper.astype(F32)
            sig = sigmoid(gate)
            silu = gate * sig
            at = 2 * j * third
            dact_all[rows, at : at + third] = (
                grad * upper * (sig + silu - silu * sig)
            ).astype(BF16)
            dact_all[rows, at + third : at + 2 * third] = (grad * silu).astype(BF16)
        hid_all[rows, :] = hid_ref[0]

        @pl.when(step == 0)
        def _():
            pltpu.make_async_copy(gate_up, gate_up, sems.at[0]).wait()

        grown = dot(dact_all[rows, :], gate_up[...], 1, 1)
        out_ref[...] = grown if first else in_ref[...] + grown

    def weight_rows(target):
        target[:, : 2 * units] = dot(xt_ref[...], dact_all[...], 1, 0).astype(BF16)
        target[:, 2 * units :] = dot(lowt_ref[...], hid_all[...], 1, 0).astype(BF16)

    @pl.when((step >= steps) & (step < steps + 2))
    def _():
        weight_rows(send_ref)

    @pl.when(step >= steps + 2)
    def _():
        weight_rows(keep_ref)


def ffn_bwd(low, saved, weights, total, xt, lowt, tile):
    plan, pieces = weights
    acts, hiddens, block = saved
    tok, width = low.shape
    units = hiddens.shape[2]
    steps = tok // tile
    quarter = width // 4
    first = total is None
    clip = lambda i: jnp.minimum(i, steps - 1)
    rows_of = lambda n: pl.BlockSpec((tile, n), lambda i: (clip(i), 0))
    slab = lambda n: pl.BlockSpec((1, tile, n), lambda i: (block, clip(i), 0))
    feature = lambda i: (jnp.where(i < steps + 2, jnp.maximum(i - steps, 0) + 2, i - steps - 2), 0)
    return pl.pallas_call(
        functools.partial(ffn_bwd_kernel, steps, plan, first),
        grid=(steps + 4,),
        in_specs=[
            rows_of(width),
            slab(2 * units),
            slab(units),
            pl.BlockSpec((quarter, tok), feature),
            pl.BlockSpec((quarter, tok), feature),
        ]
        + [ANY] * len(pieces)
        + ([] if first else [rows_of(width)]),
        out_specs=[
            rows_of(width),
            pl.BlockSpec((quarter, 3 * units), lambda i: (jnp.maximum(i - steps - 2, 0), 0)),
            pl.BlockSpec((quarter, 3 * units), lambda i: (jnp.clip(i - steps, 0, 1), 0)),
        ],
        out_shape=[
            shape_of((tok, width), F32),
            shape_of((width // 2, 3 * units), BF16),
            shape_of((width // 2, 3 * units), BF16),
        ],
        scratch_shapes=[
            pltpu.VMEM((width, 2 * units), BF16),
            pltpu.VMEM((width, units), BF16),
            pltpu.VMEM((tok, 2 * units), BF16),
            pltpu.VMEM((tok, units), BF16),
            pltpu.SemaphoreType.DMA((2,)),
        ],
        input_output_aliases={} if first else {5 + len(pieces): 0},
        compiler_params=settings(1, 60),
        cost_estimate=cost(True),
        name="ffn_bwd",
    )(low, acts, hiddens, xt, lowt, *pieces, *([] if first else [total]))


def turn_chunks(block):
    wide = block.shape[1] * 2 // 9
    thin = wide // 2
    starts = [(2 * wide, wide), (wide, wide), (0, wide)]
    starts += [(3 * wide + 2 * thin, thin), (3 * wide + thin, thin), (3 * wide, thin)]
    return jnp.concatenate([block[:, a : a + n] for a, n in starts], axis=1)


def sum_kernel(turns, *refs):
    total = None
    for ref, turn in zip(refs[:-1], turns):
        value = ref[...].astype(F32)
        value = turn_chunks(value) if turn else value
        total = value if total is None else total + value
    refs[-1][...] = total.astype(refs[-1].dtype)


def summed(terms, turns=None, dtype=BF16):
    rows, cols = terms[0].shape
    spec = pl.BlockSpec((128, cols), lambda i: (i, 0))
    return pl.pallas_call(
        functools.partial(sum_kernel, turns or [False] * len(terms)),
        grid=(rows // 128,),
        in_specs=[spec] * len(terms),
        out_specs=spec,
        out_shape=shape_of((rows, cols), dtype),
        compiler_params=settings(1, 24),
        cost_estimate=cost(False),
        name="summed",
    )(*terms)


def core_sum_kernel(info, left_ref, right_ref, *outs):
    total = (left_ref[...].astype(F32) + right_ref[...].astype(F32)).astype(BF16)
    block = pl.program_id(1)
    place = block // 2 * 2 + jnp.bitwise_xor(block % 2, info[2])
    for i, out in enumerate(outs):

        @pl.when(place == i)
        def _():
            out[...] = total


def core_sum(info, keep, came):
    groups, rows, cols = keep.shape
    spec = pl.BlockSpec((1, rows // 4, cols), lambda g, i, info: (g, i, 0))
    return pl.pallas_call(
        core_sum_kernel,
        grid_spec=pltpu.PrefetchScalarGridSpec(
            num_scalar_prefetch=1,
            grid=(groups, 4),
            in_specs=[spec] * 2,
            out_specs=[pl.BlockSpec((1, rows // 4, cols), lambda g, i, info: (g, 0, 0))] * 4,
        ),
        out_shape=[shape_of((groups, rows // 4, cols), BF16)] * 4,
        compiler_params=settings(2, 24),
        cost_estimate=cost(False),
        name="core_sum",
    )(info, keep, came)


def weight_grad_kernel(nt_ref, back0_ref, back1_ref, gt_ref, att_ref, keep_ref, send_ref):
    cols = back0_ref.shape[2]
    part, block = pl.program_id(0), pl.program_id(1)

    def rows(target, back_ref):
        target[0, :, :cols] = dot(nt_ref[...], back_ref[0], 1, 0).astype(BF16)
        target[0, :, cols:] = dot(gt_ref[...], att_ref[0], 1, 0).astype(BF16)

    for j, back_ref in enumerate((back0_ref, back1_ref)):

        @pl.when((part == 0) & (block % 2 == j))
        def _():
            rows(send_ref, back_ref)

        @pl.when((part == 1) & (block % 2 == j))
        def _():
            rows(keep_ref, back_ref)


def weight_grad(normed_t, backs, grad_t, attended):
    width, tok = normed_t.shape
    cols, feats = backs[0].shape[2], attended.shape[2]
    half = pl.BlockSpec((width // 2, tok), lambda p, k: (1 - p, 0))
    side = pl.BlockSpec((1, tok, cols), lambda p, k: (k // 2, 0, 0))
    shape = (1, width // 2, cols + feats)
    return pl.pallas_call(
        weight_grad_kernel,
        grid=(2, 4),
        in_specs=[half, side, side, half, pl.BlockSpec((1, tok, feats), lambda p, k: (k, 0, 0))],
        out_specs=[
            pl.BlockSpec(shape, lambda p, k: (jnp.where(p == 0, 0, k), 0, 0)),
            pl.BlockSpec(shape, lambda p, k: (jnp.where(p == 0, k, 3), 0, 0)),
        ],
        out_shape=[shape_of((4, width // 2, cols + feats), BF16)] * 2,
        compiler_params=settings(2, 32),
        cost_estimate=cost(True),
        name="weight_grad",
    )(normed_t, *backs, grad_t, attended)


def after(value, *others):
    return lax.optimization_barrier((value,) + others)[0]


def per_device_rows(
    tokens,
    teacher,
    lengths,
    attn_gain,
    q_weight,
    k_weight,
    v_weight,
    q_gain,
    k_gain,
    o_weight,
    ffn_gain,
    gate_weight,
    up_weight,
    down_weight,
):
    z = lax.axis_index("tp")
    ctx = lax.axis_index("ctx")
    fsdp = lax.axis_index("fsdp")
    rows_dev, tok, width = tokens.shape
    quarter = width // 4
    hd = q_gain.shape[0] * 4
    q_cols, k_cols = q_weight.shape[1], k_weight.shape[1]
    proj = q_cols + 2 * k_cols
    heads = (q_cols // hd, k_cols // hd)
    units = gate_weight.shape[1]
    slots = rows_dev * 4 * tok * 2

    def x_swap(v):
        return lax.ppermute(v, "fsdp", X_SWAP)

    def core_swap(v):
        return lax.ppermute(v, "fsdp", CORE_SWAP)

    def y_swap(v):
        return lax.ppermute(v, "ctx", Y_SWAP)

    def z_up(v):
        return lax.ppermute(v, "tp", Z_UP)

    def z_far(v):
        return lax.ppermute(v, "tp", Z_FAR)

    def z_down(v):
        return lax.ppermute(v, "tp", Z_DOWN)

    def natural(v):
        v = jnp.concatenate([v[0:1], v[2:3], v[1:2], v[3:4]], axis=0)
        v = jnp.where(fsdp % 2 == 0, v, jnp.concatenate([v[1:2], v[0:1], v[3:4], v[2:3]], axis=0))
        return jnp.where(fsdp // 2 == 0, v, jnp.concatenate([v[2:4], v[0:2]], axis=0))

    v = {}

    def sync():
        v.update(lax.optimization_barrier(dict(v)))

    length = lax.dynamic_slice_in_dim(lengths, z, 1, 0)
    info = jnp.concatenate([jnp.stack([z, fsdp, ctx]).astype(jnp.int32), length])
    w_proj = join(q_weight, k_weight, v_weight)
    proj_z = [z_up(w_proj), z_far(w_proj), z_down(w_proj)]
    proj_far = x_swap(w_proj)
    count_here = jnp.sum(lengths).astype(F32)[None]
    vector = jnp.concatenate([attn_gain, ffn_gain, q_gain, k_gain]).astype(F32)
    vector = jnp.concatenate([vector, count_here, jnp.zeros((640 - 545,), F32)])[None]
    vector = jnp.concatenate([vector, x_swap(vector)], axis=0)
    vector = jnp.concatenate([vector, core_swap(vector)], axis=0)
    w_out, w_ffn, *w_chunks = pack(info, o_weight, gate_weight, up_weight, down_weight)
    pos = (ctx * tok + jnp.arange(tok, dtype=jnp.int32)).astype(F32)
    frequency = THETA ** (-(2.0 * jnp.arange(hd // 2, dtype=F32)) / hd)
    angles = frequency[:, None] * pos[None, :]
    head_gains = natural(vector[:, 2 * quarter : 544])
    v.update(
        info=info,
        w_proj=w_proj,
        proj_far=proj_far,
        proj_z=jnp.concatenate(proj_z, axis=0),
        w_out=w_out,
        w_ffn=w_ffn,
        w_chunks=w_chunks,
        gain_one=vector[:, :quarter].reshape(1, width),
        gain_two=vector[:, quarter : 2 * quarter].reshape(1, width),
        total_count=jnp.sum(vector[:, 544]),
        gain_q=head_gains[:, : hd // 4].reshape(hd, 1),
        gain_k=head_gains[:, hd // 4 :].reshape(hd, 1),
        cos_part=jnp.cos(angles),
        sin_part=jnp.sin(angles),
    )
    sync()
    info = v["info"]

    proj_zfar = x_swap(v["proj_z"])
    one = [z_up(v["w_chunks"][0])]
    out_two = z_far(v["w_out"])
    proj_cores = [core_swap(v["w_proj"]), core_swap(v["proj_far"])]
    x_in, normed_one_t = norm_one(info, tokens, v["gain_one"], 256)
    v.update(
        proj_zfar=proj_zfar,
        proj_cores=proj_cores,
        x_in=x_in,
        normed_one_t=normed_one_t,
        one=one,
        out_two=out_two,
    )
    sync()

    proj_cores = v["proj_cores"] + [core_swap(v["proj_z"]), core_swap(v["proj_zfar"])]
    plan_proj = [[(0, 0), (1, 0), (4, 0), (5, 0)]]
    plan_proj += [[(p, k * quarter) for p in (2, 3, 6, 7)] for k in range(3)]
    weights_proj = [v["w_proj"], v["proj_far"], v["proj_z"], v["proj_zfar"]] + proj_cores
    one = v["one"] + [z_up(v["w_chunks"][1]), z_up(v["w_chunks"][2])]
    ffn_far = x_swap(v["w_ffn"])
    tables = [v[name] for name in ("cos_part", "sin_part", "gain_q", "gain_k")]

    def make(block, *then):
        normed_t = after(v["normed_one_t"], *then)
        return project(info, (plan_proj, weights_proj), normed_t, *tables, heads, block)

    theirs = [make(lambda s: 2 * (1 - s[2]))]
    got = [y_swap(theirs[0][0])]
    theirs.append(make(lambda s: 2 * (1 - s[2]) + 1, theirs[0][0]))
    got.append(y_swap(theirs[1][0]))
    mine = [make(lambda s: 2 * s[2], theirs[1][0])]
    mine.append(make(lambda s: 2 * s[2] + 1, mine[0][0]))
    v.update(
        one=one,
        ffn_far=ffn_far,
        weights_proj=weights_proj,
        mine=mine,
        theirs=theirs,
        got0=got[0],
    )
    sync()

    one_far = [x_swap(v["one"][0])]
    three = [z_down(v["w_chunks"][0])]
    own_cores = [core_swap(v["w_ffn"]), core_swap(v["ffn_far"])]
    first = attn_fwd(info, v["mine"][0][0], v["got0"], hd)
    v.update(first=first, got1=got[1], one_far=one_far, three=three, own_cores=own_cores)
    sync()

    arrived = [y_swap(v["first"][1])]
    three = v["three"] + [z_down(v["w_chunks"][1])]
    out_blocks = jnp.concatenate(
        [v["w_out"], v["one"][0][:, units:], v["out_two"], v["three"][0][:, units:]], axis=0
    )
    out_far = x_swap(out_blocks)
    one_cores = [core_swap(v["one"][0]), core_swap(v["one_far"][0])]
    second = attn_fwd(info, v["mine"][1][0], v["got1"], hd)
    v.update(
        second=second,
        arrived=arrived,
        three=three,
        out_blocks=out_blocks,
        out_far=out_far,
        one_cores=one_cores,
    )
    sync()

    arrived = v["arrived"] + [y_swap(v["second"][1])]
    three = v["three"] + [z_down(v["w_chunks"][2])]
    one_far = v["one_far"] + [x_swap(v["one"][1])]
    weights_out = [v["out_blocks"], v["out_far"]]
    weights_out += [core_swap(v["out_blocks"]), core_swap(v["out_far"])]
    one_cores = v["one_cores"] + [core_swap(v["one"][1])]
    three_cores = [core_swap(part) for part in v["three"]]
    v.update(
        arrived=arrived,
        three=three,
        one_far=one_far,
        weights_out=weights_out,
        one_cores=one_cores,
        three_cores=three_cores,
    )
    sync()

    plan_out = [[(p, k * quarter) for p in range(4)] for k in range(4)]
    two = [z_up(v["one"][0])]
    three_far = [x_swap(v["three"][0])]
    one_far = v["one_far"] + [y_swap(v["one_far"][0])]
    one_cores = v["one_cores"] + [core_swap(v["one_far"][1])]
    three_cores = v["three_cores"] + [core_swap(v["three"][2])]
    resid, normed_two, normed_two_t, attended = out_proj(
        info,
        v["x_in"],
        [v["first"][0], v["second"][0]],
        v["arrived"],
        (plan_out, v["weights_out"]),
        v["gain_two"],
        256,
    )
    v.update(
        two=two,
        three_far=three_far,
        one_far=one_far,
        one_cores=one_cores,
        three_cores=three_cores,
        resid=resid,
        normed_two=normed_two,
        normed_two_t=normed_two_t,
        attended=attended,
    )
    sync()

    plan0 = [[(i, 0, j * units) for j in range(3)] for i in range(4)]
    plan_chunks = [[(3 * p + j, 0, 0) for j in range(3)] for p in range(4)]
    scale = (slots / v["total_count"])[None]
    weights0 = [v["w_ffn"], v["ffn_far"]] + v["own_cores"]
    c0, cf, c1, cb = v["one_cores"]
    weights1 = v["one"] + v["one_far"] + [c0, c1, core_swap(v["one"][2])]
    weights1 += [cf, cb, core_swap(v["one_far"][2])]
    two = v["two"] + [z_up(v["one"][1])]
    three_far = v["three_far"] + [x_swap(v["three"][1]), y_swap(v["three_far"][0])]
    two_far = [x_swap(v["two"][0])]
    three_fars = [core_swap(v["three_far"][0])]
    acts_a, hiddens_a, sum_a = ffn_fwd(
        info,
        scale,
        v["normed_two"],
        v["resid"],
        None,
        [(plan0, weights0), (plan_chunks, weights1)],
        units,
        256,
    )
    v.update(
        scale=scale,
        weights0=weights0,
        weights1=weights1,
        two=two,
        three_far=three_far,
        two_far=two_far,
        three_fars=three_fars,
        acts_a=acts_a,
        hiddens_a=hiddens_a,
        sum_a=sum_a,
    )
    sync()

    weights3 = v["three"] + v["three_far"] + v["three_cores"] + v["three_fars"]
    weights3 += [core_swap(part) for part in v["three_far"][1:]]
    two = v["two"] + [z_up(v["one"][2])]
    two_far = v["two_far"] + [x_swap(v["two"][1]), y_swap(v["two_far"][0])]
    two_cores = [core_swap(part) for part in v["two"]]
    acts_b, hiddens_b, sum_b = ffn_fwd(
        info, v["scale"], v["normed_two"], v["sum_a"], None, [(plan_chunks, weights3)], units, 256
    )
    v.update(
        weights3=weights3,
        two=two,
        two_far=two_far,
        two_cores=two_cores,
        acts_b=acts_b,
        hiddens_b=hiddens_b,
        sum_b=sum_b,
    )
    sync()

    weights2 = v["two"] + v["two_far"] + v["two_cores"]
    weights2 += [core_swap(part) for part in v["two"][2:] + v["two_far"]]
    acts_c, hiddens_c, *results, grad_result, grad_low, grad_low_t, square = ffn_fwd(
        info, v["scale"], v["normed_two"], v["sum_b"], teacher, [(plan_chunks, weights2)], units, 256
    )
    v.update(
        weights2=weights2,
        acts_c=acts_c,
        hiddens_c=hiddens_c,
        results=results,
        grad_result=grad_result,
        grad_low=grad_low,
        grad_low_t=grad_low_t,
        square=square,
    )
    sync()

    def ffn_back(plan, weights, acts, hiddens, block, total):
        return ffn_bwd(
            v["grad_low"],
            (v[acts], v[hiddens], block),
            (plan, v[weights]),
            total,
            v["normed_two_t"],
            v["grad_low_t"],
            256,
        )

    def sum_of(k):
        return [p[0] for p in core_sum(info, v[f"keep{k}"][None], v[f"came{k}"][None])]

    turned = [False, False, True]
    one = [z_up(v["results"][0])]
    total, keep2, send2 = ffn_back(plan_chunks, "weights2", "acts_c", "hiddens_c", 0, None)
    v.update(one=one, total=total, keep2=keep2, send2=send2)
    sync()

    one = v["one"] + [z_up(v["results"][1])]
    came2 = core_swap(v["send2"])
    total, keep1, send1 = ffn_back(plan_chunks, "weights1", "acts_a", "hiddens_a", 1, v["total"])
    v.update(one=one, came2=came2, total=total, keep1=keep1, send1=send1)
    sync()

    out_three = [z_down(v["results"][0])]
    came1 = core_swap(v["send1"])
    sum2 = sum_of(2)
    far_t2 = x_swap(sum2[3])
    total, keep3, send3 = ffn_back(
        plan_chunks, "weights3", "acts_b", "hiddens_b", 0, after(v["total"], sum2[0])
    )
    v.update(
        out_three=out_three,
        came1=came1,
        sum2=sum2,
        far_t2=far_t2,
        total=total,
        keep3=keep3,
        send3=send3,
    )
    sync()

    out_three = v["out_three"] + [z_down(v["results"][1])]
    came3 = core_swap(v["send3"])
    far_h2 = x_swap(v["sum2"][2])
    there2 = y_swap(summed([v["sum2"][1], v["far_t2"]]))
    sum1 = sum_of(1)
    total, keep0, send0 = ffn_back(
        plan0, "weights0", "acts_a", "hiddens_a", 0, after(v["total"], sum1[0])
    )
    v.update(
        out_three=out_three,
        came3=came3,
        far_h2=far_h2,
        there2=there2,
        sum1=sum1,
        total=total,
        keep0=keep0,
        send0=send0,
    )
    sync()

    came0 = core_swap(v["send0"])
    far_t1 = x_swap(v["sum1"][3])
    down2 = z_down(summed([v["sum2"][0], v["far_h2"], v["there2"]], turned))
    sum3 = sum_of(3)
    grad_resid, grad_attn_t, a0, a1, b0, b1, gain_two_sum = norm_two_back(
        info,
        after(v["total"], sum3[0]),
        v["resid"],
        v["grad_result"],
        v["gain_two"],
        (plan_out, v["weights_out"]),
        256,
    )
    grad_got = [y_swap(b0), y_swap(b1)]
    v.update(
        came0=came0,
        far_t1=far_t1,
        down2=down2,
        sum3=sum3,
        grad_resid=grad_resid,
        grad_attn_t=grad_attn_t,
        grad_mine=[a0, a1],
        gain_two_sum=gain_two_sum,
        grad_got0=grad_got[0],
    )
    sync()

    def attn_back(j, grad):
        out, got_ref = v["first" if j == 0 else "second"], v[f"got{j}"]
        return attn_bwd(
            info, v["mine"][j][0], got_ref, out[0], out[1], grad, v[f"grad_got{j}"], out[2], hd
        )

    two = [z_up(v["one"][0])]
    far_h1 = x_swap(v["sum1"][2])
    there1 = y_swap(summed([v["sum1"][1], v["far_t1"]]))
    far_t3 = x_swap(v["sum3"][3])
    sum0 = sum_of(0)
    back0 = attn_back(0, after(v["grad_mine"][0], sum0[0]))
    v.update(
        out_two=two,
        far_h1=far_h1,
        there1=there1,
        far_t3=far_t3,
        sum0=sum0,
        back0=back0,
        grad_got1=grad_got[1],
    )
    sync()

    two = v["out_two"] + [z_up(v["one"][1])]
    heads0 = y_swap(v["back0"][1])
    far_h3 = x_swap(v["sum3"][2])
    far_t0 = x_swap(v["sum0"][3])
    there3 = summed([v["sum3"][1], v["far_t3"]])
    two_down = summed(
        [v["sum1"][0], v["far_h1"], v["there1"], v["down2"]], [False, False, True, False]
    )
    there3_got = y_swap(there3)
    two_down_got = z_down(two_down)
    back1 = attn_back(1, after(v["grad_mine"][1], there3, two_down))
    v.update(
        out_two=two, heads0=heads0, far_h3=far_h3, far_t0=far_t0, there3=there3_got, back1=back1
    )
    sync()

    heads1 = y_swap(v["back1"][1])
    far_h0 = x_swap(v["sum0"][2])
    up3 = z_up(summed([v["sum3"][0], v["far_h3"], v["there3"]], turned))
    tables = [v[name] for name in ("cos_part", "sin_part", "gain_q", "gain_k")]
    head0 = head_back(
        info, v["back0"][0], v["heads0"], v["mine"][0][1], v["theirs"][0][1], *tables, heads
    )
    v.update(heads1=heads1, two_down=two_down_got, head0=head0)
    sync()

    there0 = y_swap(summed([v["sum0"][1], v["far_t0"]]))
    head1 = head_back(
        info, v["back1"][0], v["heads1"], v["mine"][1][1], v["theirs"][1][1], *tables, heads
    )
    *tokens_low, gain_one_sum = norm_one_back(
        info,
        [v["head0"][0], head1[0]],
        (plan_proj, v["weights_proj"]),
        v["x_in"],
        v["grad_resid"],
        v["gain_one"],
        tok // 4,
    )
    v.update(head1=head1, tokens_low=tokens_low, gain_one_sum=gain_one_sum, up3=up3)
    v.update(there0=there0, far_h0=far_h0)
    sync()

    def place(out, parts, k, first):
        row = lax.rem(z - k + 4, 4)
        for j, part in enumerate(parts):
            at = (first + j) * part.shape[0]
            out = lax.dynamic_update_slice(out, part.astype(out.dtype)[None], (row, at, 0))
        return out

    v.update(out_one=v["one"])
    quarters = v["tokens_low"]
    one = [z_up(quarters[0])]
    keep, send = weight_grad(
        v["normed_one_t"], [v["head0"][0], v["head1"][0]], v["grad_attn_t"], v["attended"]
    )
    gain_heads = v["head0"][1] + v["head1"][1]
    vector = jnp.concatenate(
        [
            natural(v["gain_one_sum"].reshape(4, quarter)).reshape(1, width),
            natural(v["gain_two_sum"].reshape(4, quarter)).reshape(1, width),
            gain_heads[:, 0].reshape(1, hd),
            gain_heads[:, 1].reshape(1, hd),
            jnp.sum(v["square"]).reshape(1, 1),
            jnp.zeros((1, 127), F32),
        ],
        axis=1,
    )
    vector = vector + core_swap(vector)
    v.update(one=one, keep=keep, came=core_swap(send))
    v.update(vector=vector)
    sync()

    one = v["one"] + [z_up(part) for part in v["tokens_low"][1:3]]
    rows = quarter // 2
    flat = lambda a: a.reshape(4 * rows, a.shape[-1])
    sums = [flat(p) for p in core_sum(info, v["keep"], v["came"])]
    far_t = x_swap(sums[3])
    part0 = summed([v["sum0"][0], v["far_h0"], v["there0"]], turned)
    ffn_sum = summed([part0, v["two_down"], v["up3"]], None, F32)
    vector = v["vector"] + x_swap(v["vector"])
    v.update(one=one, sums=sums, far_t=far_t, ffn_sum=ffn_sum, vector=vector)
    sync()

    one = v["one"] + [z_up(v["tokens_low"][3])]
    three = [z_down(v["tokens_low"][0])]
    far_h = x_swap(v["sums"][2])
    there = y_swap(summed([v["sums"][1], v["far_t"]]))
    vector = v["vector"] + y_swap(v["vector"])
    output = jnp.zeros((rows_dev, tok, width), BF16)
    for k, parts in enumerate((v["results"], v["out_one"], v["out_two"], v["out_three"])):
        output = place(output, parts, k, 0)
    v.update(one=one, three=three, far_h=far_h, there=there, vector=vector, output=output)
    sync()

    three = v["three"] + [z_down(v["tokens_low"][1])]
    parts = summed([v["sums"][0], v["far_h"], v["there"]])
    parts = [parts[k * rows : (k + 1) * rows] for k in range(4)]
    parts = [parts[0], z_down(parts[1]), z_far(parts[2]), z_up(parts[3])]
    ffn_other = y_swap(v["ffn_sum"])
    grad = place(jnp.zeros((rows_dev, tok, width), F32), v["tokens_low"], 0, 0)
    v.update(three=three, parts=parts, grad=grad)
    sync()

    three = v["three"] + [z_down(part) for part in v["tokens_low"][2:]]
    attn_sum = summed(v["parts"], None, F32)
    attn_other = y_swap(attn_sum)
    vector = v["vector"] + lax.ppermute(v["vector"], "tp", Z_NEAR)
    grad = place(v["grad"], v["one"], 1, 0)
    v.update(three=three, attn_sum=attn_sum, attn_other=attn_other, vector=vector, grad=grad)
    sync()

    two = [z_up(part) for part in v["one"][:2]]
    vector = v["vector"] + lax.ppermute(v["vector"], "tp", Z_FAR)
    grad = place(v["grad"], v["three"], 3, 0)
    v.update(two=two, vector=vector, grad=grad, ffn_other=ffn_other)
    sync()

    two = [z_up(part) for part in v["one"][2:]]
    tokens_grad = place(place(v["grad"], v["two"], 2, 0), two, 2, 2)
    output = v["output"]
    sums = v["vector"][0]

    def finish(own, other):
        return jnp.concatenate(
            [jnp.where(ctx == 0, own, other), jnp.where(ctx == 0, other, own)], axis=0
        )

    ffn_grad = finish(v["ffn_sum"], turn_chunks(v["ffn_other"]))
    attn_grad = finish(v["attn_sum"], v["attn_other"])
    teacher_loss = sums[2 * width + 2 * hd] / (v["total_count"] * width)

    def own_part(at, size):
        return lax.dynamic_slice_in_dim(sums, at + fsdp * (size // 4), size // 4, 0)

    third = units // 3

    def columns(first):
        starts = [first(j) for j in range(3)]
        parts = [ffn_grad[:, s : s + third] for s in starts]
        return jnp.concatenate(
            [jnp.where(ctx == 0, parts[0], parts[2]), parts[1], jnp.where(ctx == 0, parts[2], parts[0])],
            axis=1,
        )

    return (
        output,
        teacher_loss,
        tokens_grad,
        own_part(0, width),
        attn_grad[:, :q_cols],
        attn_grad[:, q_cols : q_cols + k_cols],
        attn_grad[:, q_cols + k_cols : proj],
        own_part(2 * width, hd),
        own_part(2 * width + hd, hd),
        attn_grad[:, proj:].T,
        own_part(width, width),
        columns(lambda j: 2 * j * third),
        columns(lambda j: (2 * j + 1) * third),
        columns(lambda j: 2 * units + j * third).T,
    )


def solution(mesh):
    return jax.shard_map(
        per_device_rows if fits(mesh) else per_device_any,
        mesh=mesh,
        in_specs=(
            P("fsdp", "ctx", None),
            P("fsdp", "ctx", None),
            P("fsdp"),
            P("fsdp"),
            P("fsdp", "tp"),
            P("fsdp", "tp"),
            P("fsdp", "tp"),
            P("fsdp"),
            P("fsdp"),
            P("tp", "fsdp"),
            P("fsdp"),
            P("fsdp", "tp"),
            P("fsdp", "tp"),
            P("tp", "fsdp"),
        ),
        out_specs=(
            P("fsdp", "ctx", None),
            P(),
            P("fsdp", "ctx", None),
            P("fsdp"),
            P("fsdp", "tp"),
            P("fsdp", "tp"),
            P("fsdp", "tp"),
            P("fsdp"),
            P("fsdp"),
            P("tp", "fsdp"),
            P("fsdp"),
            P("fsdp", "tp"),
            P("fsdp", "tp"),
            P("tp", "fsdp"),
        ),
        check_vma=False,
    )
```

```python
import functools
import math

import jax
import jax.numpy as jnp
from jax import lax
from jax.experimental import pallas as pl
from jax.experimental.pallas import tpu as pltpu
from jax.sharding import PartitionSpec as P

EPS = 1e-05
THETA = 1000000.0
NEGATIVE = -1e30


def rms_scale(field_in, gain_vec):
    return (
        field_in * lax.rsqrt(jnp.mean(field_in * field_in, axis=-1, keepdims=True) + EPS) * gain_vec
    )


def rotate(field_in, positions):
    half_dim = field_in.shape[-1] // 2
    frequency = THETA ** (-(2.0 * jnp.arange(half_dim, dtype=jnp.float32)) / field_in.shape[-1])
    angles = positions[:, None] * frequency[None, :]
    cos_part = jnp.cos(angles)[:, None, :]
    sin_part = jnp.sin(angles)[:, None, :]
    lower_half = field_in[..., :half_dim]
    upper_half = field_in[..., half_dim:]
    return jnp.concatenate(
        [
            lower_half * cos_part - upper_half * sin_part,
            upper_half * cos_part + lower_half * sin_part,
        ],
        axis=-1,
    )


def linear(left_mat, right_mat):
    return jnp.dot(left_mat, right_mat, preferred_element_type=jnp.float32)


def linear_left(left_mat, right_mat):
    return lax.dot_general(
        left_mat, right_mat, (((0,), (0,)), ((), ())), preferred_element_type=jnp.float32
    )


def linear_right(left_mat, right_mat):
    return lax.dot_general(
        left_mat, right_mat, (((1,), (1,)), ((), ())), preferred_element_type=jnp.float32
    )


def swiglu(gate_act, up_act):
    return jax.nn.silu(gate_act) * up_act


def per_device_any(
    tokens,
    teacher,
    lengths,
    attn_gain,
    q_weight,
    k_weight,
    v_weight,
    q_gain,
    k_gain,
    o_weight,
    ffn_gain,
    gate_weight,
    up_weight,
    down_weight,
):
    (
        gain_one,
        w_query,
        w_key,
        w_value,
        gain_query,
        gain_key,
        w_output,
        gain_two,
        w_gate,
        w_upper,
        w_down,
    ) = (
        lax.all_gather(attn_gain, "fsdp", axis=0, tiled=True),
        lax.all_gather(q_weight, "fsdp", axis=0, tiled=True),
        lax.all_gather(k_weight, "fsdp", axis=0, tiled=True),
        lax.all_gather(v_weight, "fsdp", axis=0, tiled=True),
        lax.all_gather(q_gain, "fsdp", axis=0, tiled=True),
        lax.all_gather(k_gain, "fsdp", axis=0, tiled=True),
        lax.all_gather(o_weight, "fsdp", axis=1, tiled=True),
        lax.all_gather(ffn_gain, "fsdp", axis=0, tiled=True),
        lax.all_gather(gate_weight, "fsdp", axis=0, tiled=True),
        lax.all_gather(up_weight, "fsdp", axis=0, tiled=True),
        lax.all_gather(down_weight, "fsdp", axis=1, tiled=True),
    )
    rows_dev, block_len, model_width = tokens.shape
    count_tok = rows_dev * block_len
    head_dim = gain_query.shape[0]
    q_heads = w_query.shape[1] // head_dim
    kv_heads = w_key.shape[1] // head_dim
    group_size = q_heads // kv_heads
    score_scale = head_dim ** (-0.5)
    row_len = block_len * lax.axis_size("ctx")
    key_block = math.gcd(row_len, 512)
    block_start = lax.axis_index("ctx") * block_len
    tiles_used = (block_start + block_len + key_block - 1) // key_block
    slot_pos = block_start + jnp.arange(block_len, dtype=jnp.int32)
    positions = slot_pos.astype(jnp.float32)
    valid = (slot_pos[None, :] < lengths[:, None]).astype(jnp.float32)
    slots = count_tok * lax.axis_size("fsdp") * lax.axis_size("ctx")
    gain_two_f = gain_two.astype(jnp.float32)
    gain_one_f = gain_one.astype(jnp.float32)
    inputs = tokens.astype(jnp.float32)
    normed_one, back_one = jax.vjp(rms_scale, inputs, gain_one_f)
    normed_low = normed_one.astype(jnp.bfloat16).reshape(count_tok, model_width)
    query_raw = linear(normed_low, w_query)
    key_raw = linear(normed_low, w_key)
    value_raw = linear(normed_low, w_value)

    def heads_post(raw_heads, gain_vec):
        shaped = raw_heads.reshape(rows_dev, block_len, -1, head_dim)
        return rotate(rms_scale(shaped, gain_vec), positions)

    query_rot, query_back = jax.vjp(heads_post, query_raw, gain_query.astype(jnp.float32))
    key_rot, key_back = jax.vjp(heads_post, key_raw, gain_key.astype(jnp.float32))
    queries = query_rot.astype(jnp.bfloat16).reshape(
        rows_dev, block_len, kv_heads, group_size, head_dim
    )
    key_rows = key_rot.astype(jnp.bfloat16).reshape(rows_dev, block_len, kv_heads * head_dim)
    values = value_raw.astype(jnp.bfloat16).reshape(rows_dev, block_len, kv_heads * head_dim)
    keys_all, values_all = (
        lax.all_gather(key_rows, "ctx", axis=1, tiled=True),
        lax.all_gather(values, "ctx", axis=1, tiled=True),
    )

    def key_tile(tile_index):
        tile_start = tile_index * key_block
        key_pos = tile_start + jnp.arange(key_block, dtype=jnp.int32)
        key_part = lax.dynamic_slice_in_dim(keys_all, tile_start, key_block, 1).reshape(
            rows_dev, key_block, kv_heads, head_dim
        )
        value_part = lax.dynamic_slice_in_dim(values_all, tile_start, key_block, 1).reshape(
            rows_dev, key_block, kv_heads, head_dim
        )
        scores = (
            jnp.einsum("rqhgd,rkhd->rhgqk", queries, key_part, preferred_element_type=jnp.float32)
            * score_scale
        )
        allowed = (key_pos[None, None, :] <= slot_pos[None, :, None]) & (
            key_pos[None, None, :] < lengths[:, None, None]
        )
        return (tile_start, scores, allowed[:, None, None], key_part, value_part)

    stat_shape = (rows_dev, kv_heads, group_size, block_len)

    def stats_step(tile_index, carried):
        running_max, running_sum = carried
        tile_start, scores, allowed, key_part, value_part = key_tile(tile_index)
        masked = jnp.where(allowed, scores, NEGATIVE)
        new_max = jnp.maximum(running_max, jnp.max(masked, axis=-1))
        terms = jnp.where(allowed, jnp.exp(masked - new_max[..., None]), 0.0)
        return (new_max, running_sum * jnp.exp(running_max - new_max) + jnp.sum(terms, axis=-1))

    running_max, running_sum = lax.fori_loop(
        0,
        tiles_used,
        stats_step,
        (jnp.full(stat_shape, NEGATIVE, jnp.float32), jnp.zeros(stat_shape, jnp.float32)),
    )
    log_total = running_max + jnp.log(running_sum)
    out_shape = (rows_dev, block_len, kv_heads, group_size, head_dim)

    def value_step(tile_index, carried):
        rounded_out, exact_out = carried
        tile_start, scores, allowed, key_part, value_part = key_tile(tile_index)
        tile_probs = jnp.where(allowed, jnp.exp(scores - log_total[..., None]), 0.0)
        rounded_out = rounded_out + jnp.einsum(
            "rhgqk,rkhd->rqhgd",
            tile_probs.astype(jnp.bfloat16),
            value_part,
            preferred_element_type=jnp.float32,
        )
        exact_out = exact_out + jnp.einsum(
            "rhgqk,rkhd->rqhgd", tile_probs, value_part.astype(jnp.float32)
        )
        return (rounded_out, exact_out)

    rounded_out, exact_out = lax.fori_loop(
        0,
        tiles_used,
        value_step,
        (jnp.zeros(out_shape, jnp.float32), jnp.zeros(out_shape, jnp.float32)),
    )
    attended = rounded_out.astype(jnp.bfloat16).reshape(count_tok, q_heads * head_dim)
    attn_total = lax.psum(linear(attended, w_output), "tp")
    resid = inputs + attn_total.reshape(rows_dev, block_len, model_width)
    normed_two, back_two = jax.vjp(rms_scale, resid, gain_two_f)
    normed_second = normed_two.astype(jnp.bfloat16).reshape(count_tok, model_width)
    gate_act = linear(normed_second, w_gate)
    up_act = linear(normed_second, w_upper)
    hidden_full, back_glu = jax.vjp(swiglu, gate_act, up_act)
    hidden = hidden_full.astype(jnp.bfloat16)
    ffn_total = lax.psum(linear(hidden, w_down), "tp")
    result = resid + ffn_total.reshape(rows_dev, block_len, model_width)
    error_value = result - teacher.astype(jnp.float32)
    valid_col = valid[..., None]
    total_square, total_count = lax.psum(
        (jnp.sum(valid_col * error_value * error_value), jnp.sum(valid)), ("fsdp", "ctx")
    )
    teacher_loss = total_square / (total_count * model_width)
    grad_result = valid_col * error_value * (slots / total_count)
    grad_low = grad_result.astype(jnp.bfloat16).reshape(count_tok, model_width)
    grad_down = linear_left(hidden, grad_low)
    grad_hidden = linear_right(grad_low, w_down)
    grad_gate_full, grad_up_full = back_glu(grad_hidden)
    grad_gate = grad_gate_full.astype(jnp.bfloat16)
    grad_up = grad_up_full.astype(jnp.bfloat16)
    grad_wgate = linear_left(normed_second, grad_gate)
    grad_wup = linear_left(normed_second, grad_up)
    normed_two_part = linear_right(grad_gate, w_gate) + linear_right(grad_up, w_upper)
    grad_normed_two = lax.psum(normed_two_part, "tp")
    grad_resid_norm, grad_gain_two = back_two(
        grad_normed_two.reshape(rows_dev, block_len, model_width)
    )
    grad_resid = grad_result + grad_resid_norm
    grad_attn_low = grad_resid.astype(jnp.bfloat16).reshape(count_tok, model_width)
    grad_woutput = linear_left(attended, grad_attn_low)
    grad_attended = linear_right(grad_attn_low, w_output).astype(jnp.bfloat16).reshape(out_shape)
    delta = jnp.einsum("rqhgd,rqhgd->rhgq", grad_attended.astype(jnp.float32), exact_out)
    full_shape = (rows_dev, row_len, kv_heads * head_dim)

    def grad_step(tile_index, carried):
        grad_queries, grad_keys, grad_values = carried
        tile_start, scores, allowed, key_part, value_part = key_tile(tile_index)
        tile_probs = jnp.where(allowed, jnp.exp(scores - log_total[..., None]), 0.0)
        grad_probs = jnp.einsum(
            "rqhgd,rkhd->rhgqk", grad_attended, value_part, preferred_element_type=jnp.float32
        )
        grad_scores = (tile_probs * (grad_probs - delta[..., None])).astype(jnp.bfloat16)
        grad_queries = (
            grad_queries
            + jnp.einsum(
                "rhgqk,rkhd->rqhgd", grad_scores, key_part, preferred_element_type=jnp.float32
            )
            * score_scale
        )
        key_term = (
            jnp.einsum(
                "rhgqk,rqhgd->rkhd", grad_scores, queries, preferred_element_type=jnp.float32
            )
            * score_scale
        )
        value_term = jnp.einsum(
            "rhgqk,rqhgd->rkhd",
            tile_probs.astype(jnp.bfloat16),
            grad_attended,
            preferred_element_type=jnp.float32,
        )
        grad_keys = lax.dynamic_update_slice_in_dim(
            grad_keys, key_term.reshape(rows_dev, key_block, kv_heads * head_dim), tile_start, 1
        )
        grad_values = lax.dynamic_update_slice_in_dim(
            grad_values, value_term.reshape(rows_dev, key_block, kv_heads * head_dim), tile_start, 1
        )
        return (grad_queries, grad_keys, grad_values)

    grad_queries, grad_keys, grad_values = lax.fori_loop(
        0,
        tiles_used,
        grad_step,
        (
            jnp.zeros(out_shape, jnp.float32),
            jnp.zeros(full_shape, jnp.float32),
            jnp.zeros(full_shape, jnp.float32),
        ),
    )
    key_grad, value_grad = (
        lax.psum_scatter(grad_keys, "ctx", scatter_dimension=1, tiled=True),
        lax.psum_scatter(grad_values, "ctx", scatter_dimension=1, tiled=True),
    )
    grad_query_raw, grad_gain_query = query_back(
        grad_queries.reshape(rows_dev, block_len, q_heads, head_dim)
    )
    grad_key_raw, grad_gain_key = key_back(
        key_grad.reshape(rows_dev, block_len, kv_heads, head_dim)
    )
    query_low = grad_query_raw.astype(jnp.bfloat16)
    key_low = grad_key_raw.astype(jnp.bfloat16)
    value_low = value_grad.reshape(count_tok, kv_heads * head_dim).astype(jnp.bfloat16)
    grad_wquery = linear_left(normed_low, query_low)
    grad_wkey = linear_left(normed_low, key_low)
    grad_wvalue = linear_left(normed_low, value_low)
    normed_part = (
        linear_right(query_low, w_query)
        + linear_right(key_low, w_key)
        + linear_right(value_low, w_value)
    )
    grad_normed_one, grad_gain_query, grad_gain_key = lax.psum(
        (normed_part, grad_gain_query, grad_gain_key), "tp"
    )
    grad_input_norm, grad_gain_one = back_one(
        grad_normed_one.reshape(rows_dev, block_len, model_width)
    )
    tokens_grad = grad_resid + grad_input_norm
    partials = (
        grad_gain_one,
        grad_wquery,
        grad_wkey,
        grad_wvalue,
        grad_gain_query,
        grad_gain_key,
        grad_woutput,
        grad_gain_two,
        grad_wgate,
        grad_wup,
        grad_down,
    )
    pieces = (
        lax.psum_scatter(partials[0], ("fsdp", "ctx"), scatter_dimension=0, tiled=True),
        lax.psum_scatter(partials[1], ("fsdp", "ctx"), scatter_dimension=0, tiled=True),
        lax.psum_scatter(partials[2], ("fsdp", "ctx"), scatter_dimension=0, tiled=True),
        lax.psum_scatter(partials[3], ("fsdp", "ctx"), scatter_dimension=0, tiled=True),
        lax.psum_scatter(partials[4], ("fsdp", "ctx"), scatter_dimension=0, tiled=True),
        lax.psum_scatter(partials[5], ("fsdp", "ctx"), scatter_dimension=0, tiled=True),
        lax.psum_scatter(partials[6], ("fsdp", "ctx"), scatter_dimension=1, tiled=True),
        lax.psum_scatter(partials[7], ("fsdp", "ctx"), scatter_dimension=0, tiled=True),
        lax.psum_scatter(partials[8], ("fsdp", "ctx"), scatter_dimension=0, tiled=True),
        lax.psum_scatter(partials[9], ("fsdp", "ctx"), scatter_dimension=0, tiled=True),
        lax.psum_scatter(partials[10], ("fsdp", "ctx"), scatter_dimension=1, tiled=True),
    )
    summed = (
        lax.all_gather(pieces[0], "ctx", axis=0, tiled=True),
        lax.all_gather(pieces[1], "ctx", axis=0, tiled=True),
        lax.all_gather(pieces[2], "ctx", axis=0, tiled=True),
        lax.all_gather(pieces[3], "ctx", axis=0, tiled=True),
        lax.all_gather(pieces[4], "ctx", axis=0, tiled=True),
        lax.all_gather(pieces[5], "ctx", axis=0, tiled=True),
        lax.all_gather(pieces[6], "ctx", axis=1, tiled=True),
        lax.all_gather(pieces[7], "ctx", axis=0, tiled=True),
        lax.all_gather(pieces[8], "ctx", axis=0, tiled=True),
        lax.all_gather(pieces[9], "ctx", axis=0, tiled=True),
        lax.all_gather(pieces[10], "ctx", axis=1, tiled=True),
    )
    return (
        result.astype(jnp.bfloat16),
        teacher_loss,
        tokens_grad,
        summed[0],
        summed[1],
        summed[2],
        summed[3],
        summed[4],
        summed[5],
        summed[6],
        summed[7],
        summed[8],
        summed[9],
        summed[10],
    )


BF16 = jnp.bfloat16
F32 = jnp.float32
LOG2E = math.log2(math.e)
X_SWAP = [(0, 2), (2, 0), (1, 3), (3, 1)]
CORE_SWAP = [(0, 1), (1, 0), (2, 3), (3, 2)]
Y_SWAP = [(0, 1), (1, 0)]
Z_UP = [(0, 1), (1, 2), (2, 3), (3, 0)]
Z_DOWN = [(0, 3), (1, 0), (2, 1), (3, 2)]
Z_NEAR = [(0, 1), (1, 0), (2, 3), (3, 2)]
Z_FAR = [(0, 2), (2, 0), (1, 3), (3, 1)]
MASKS = (0, 2, 1, 3)
ANY = pl.BlockSpec(memory_space=pl.ANY)
SMEM = pl.BlockSpec(memory_space=pltpu.SMEM)


def fits(mesh):
    return dict(mesh.shape) == {"fsdp": 4, "ctx": 2, "tp": 4}


def dot(left, right, left_dim, right_dim):
    return lax.dot_general(
        left, right, (((left_dim,), (right_dim,)), ((), ())), preferred_element_type=F32
    )


def sigmoid(v):
    return 0.5 * jnp.tanh(0.5 * v) + 0.5


def whole(shape):
    zeros = (0,) * len(shape)
    return pl.BlockSpec(shape, lambda *_: zeros, pipeline_mode=pl.Buffered(1))


def settings(dims, mib):
    return pltpu.CompilerParams(
        dimension_semantics=("arbitrary",) * dims, vmem_limit_bytes=mib << 20
    )


def shape_of(shape, dtype):
    return jax.ShapeDtypeStruct(shape, dtype)


def cost(large):
    size = 1 << 42 if large else 1 << 10
    return pl.CostEstimate(flops=size, bytes_accessed=size >> 12, transcendentals=0)


def pack_kernel(info, o_in, g_in, u_in, d_in, *refs):
    out_ref, ffn_ref, *chunk_refs, others_ref, o_ref, g_ref, u_ref, d_ref, sems = refs
    ctx = info[2]
    pairs = ((o_in, o_ref), (g_in, g_ref), (u_in, u_ref), (d_in, d_ref))
    copies = [pltpu.make_async_copy(a, b, sems.at[i]) for i, (a, b) in enumerate(pairs)]
    for copy in copies:
        copy.start()
    for copy in copies:
        copy.wait()
    out_ref[...] = o_ref[...].astype(F32).T.astype(BF16)
    third = g_ref.shape[1] // 3
    for j in range(3):
        at = pl.multiple_of(jnp.where(ctx == 0, j, 2 - j) * third, third)
        parts = [
            g_ref[:, pl.ds(at, third)],
            u_ref[:, pl.ds(at, third)],
            d_ref[pl.ds(at, third), :].astype(F32).T.astype(BF16),
        ]
        for i, part in enumerate(parts):
            chunk_refs[j][:, i * third : (i + 1) * third] = part
            if j:
                others_ref[:, (3 * j - 3 + i) * third : (3 * j - 2 + i) * third] = part
            ffn_ref[:, (3 * j + i) * third : (3 * j + i + 1) * third] = part


def pack(info, o, g, u, d):
    rows, units = g.shape
    feats = o.shape[0]
    widths = (feats, 3 * units, units, units, units, 2 * units)
    return pl.pallas_call(
        pack_kernel,
        in_specs=[SMEM] + [ANY] * 4,
        out_specs=[pl.BlockSpec(memory_space=pltpu.VMEM)] * 6,
        out_shape=[shape_of((rows, n), BF16) for n in widths],
        scratch_shapes=[pltpu.VMEM(a.shape, BF16) for a in (o, g, u, d)]
        + [pltpu.SemaphoreType.DMA((4,))],
        compiler_params=pltpu.CompilerParams(vmem_limit_bytes=24 << 20),
        cost_estimate=cost(False),
        name="pack",
    )(info, o, g, u, d)


def join_kernel(q_ref, k_ref, v_ref, out_ref):
    at = 0
    for ref in (q_ref, k_ref, v_ref):
        out_ref[:, at : at + ref.shape[1]] = ref[...]
        at += ref.shape[1]


def join(q, k, v):
    return pl.pallas_call(
        join_kernel,
        out_shape=shape_of((q.shape[0], q.shape[1] + k.shape[1] + v.shape[1]), BF16),
        compiler_params=pltpu.CompilerParams(vmem_limit_bytes=8 << 20),
        cost_estimate=cost(False),
        name="join",
    )(q, k, v)


def norm_one_kernel(info, tok_ref, gain_ref, x_ref, nt_ref, x32):
    quarter = x_ref.shape[1] // 4
    for p, mask in enumerate(MASKS):
        at = pl.multiple_of(jnp.bitwise_xor(info[1], mask) * quarter, quarter)
        part = tok_ref[0, :, pl.ds(at, quarter)]
        x_ref[:, p * quarter : (p + 1) * quarter] = part
        x32[:, p * quarter : (p + 1) * quarter] = part.astype(F32)
    x = x32[...]
    rho = lax.rsqrt(jnp.mean(x * x, axis=-1, keepdims=True) + EPS)
    nt_ref[...] = (x * rho * gain_ref[...]).T.astype(BF16)


def norm_one(info, tokens, gain, tile):
    _, tok, width = tokens.shape
    return pl.pallas_call(
        norm_one_kernel,
        grid_spec=pltpu.PrefetchScalarGridSpec(
            num_scalar_prefetch=1,
            grid=(tok // tile,),
            in_specs=[
                pl.BlockSpec((1, tile, width), lambda i, info: (info[0], i, 0)),
                pl.BlockSpec((1, width), lambda i, info: (0, 0)),
            ],
            out_specs=[
                pl.BlockSpec((tile, width), lambda i, info: (i, 0)),
                pl.BlockSpec((width, tile), lambda i, info: (0, i)),
            ],
            scratch_shapes=[pltpu.VMEM((tile, width), F32)],
        ),
        out_shape=[shape_of((tok, width), BF16), shape_of((width, tok), BF16)],
        compiler_params=settings(1, 24),
        cost_estimate=cost(False),
        name="norm_one",
    )(info, tokens, gain)


def proj_kernel(heads, block, plan, count, info, *refs):
    nt_ref, cos_ref, sin_ref, qg_ref, kg_ref, rot_ref, raw_ref, w_ref, sem = refs[count:]
    rows = w_ref.shape[0] // 4

    @pl.when(pl.program_id(0) == 0)
    def _():
        for k in range(4):

            @pl.when(block(info) == k)
            def _():
                for p, (piece, row) in enumerate(plan[k]):
                    src = refs[piece].at[pl.ds(row, rows)]
                    pltpu.make_async_copy(src, w_ref.at[pl.ds(p * rows, rows)], sem).start()

        pltpu.make_async_copy(w_ref, w_ref, sem).wait()

    hd = qg_ref.shape[0]
    half = hd // 2
    raw = dot(w_ref[...], nt_ref[...], 0, 0)
    cos_part, sin_part = cos_ref[...], sin_ref[...]
    heads_q, heads_k = heads
    raw_ref[...] = raw.astype(BF16)
    for h in range(heads_q + heads_k):
        v = raw[h * hd : (h + 1) * hd]
        rho = lax.rsqrt(jnp.mean(v * v, axis=0, keepdims=True) + EPS)
        v = v * rho * (qg_ref[...] if h < heads_q else kg_ref[...])
        a, b = v[:half], v[half:]
        rot_ref[h * hd : h * hd + half, :] = (a * cos_part - b * sin_part).astype(BF16)
        rot_ref[h * hd + half : (h + 1) * hd, :] = (b * cos_part + a * sin_part).astype(BF16)
    at = (heads_q + heads_k) * hd
    rot_ref[at:, :] = raw[at:].astype(BF16)


def project(info, weights, normed_t, cos_part, sin_part, gain_q, gain_k, heads, block):
    plan, pieces = weights
    width, tok = normed_t.shape
    cols = pieces[0].shape[1]
    tile = min(512, tok)
    const = lambda a: pl.BlockSpec(a.shape, lambda i, info: (0, 0))
    tab = lambda a: pl.BlockSpec((a.shape[0], tile), lambda i, info: (0, i))
    return pl.pallas_call(
        functools.partial(proj_kernel, heads, block, plan, len(pieces)),
        grid_spec=pltpu.PrefetchScalarGridSpec(
            num_scalar_prefetch=1,
            grid=(tok // tile,),
            in_specs=[ANY] * len(pieces)
            + [tab(normed_t), tab(cos_part), tab(sin_part), const(gain_q), const(gain_k)],
            out_specs=[pl.BlockSpec((cols, tile), lambda i, info: (0, i))] * 2,
            scratch_shapes=[pltpu.VMEM((width, cols), BF16), pltpu.SemaphoreType.DMA],
        ),
        out_shape=[shape_of((cols, tok), BF16), shape_of((cols, tok), BF16)],
        compiler_params=settings(1, 24),
        cost_estimate=cost(False),
        name="project",
    )(info, *pieces, normed_t, cos_part, sin_part, gain_q, gain_k)


def head_back_kernel(
    heads, info, dm_ref, dt_ref, rm_ref, rt_ref, cos_ref, sin_ref, qg_ref, kg_ref, out_ref, gg_ref
):
    step, part = pl.program_id(0), pl.program_id(1)
    hd = qg_ref.shape[0]
    half = hd // 2
    heads_q, heads_k = heads
    cos_part, sin_part = cos_ref[...], sin_ref[...]
    tile = cos_part.shape[1]

    @pl.when((step == 0) & (part == 0))
    def _():
        gg_ref[...] = jnp.zeros_like(gg_ref)

    def work(d_ref, r_ref):
        gain_q = jnp.zeros((hd, 1), F32)
        gain_k = jnp.zeros((hd, 1), F32)
        done = []
        for h in range(heads_q + heads_k):
            is_q = h < heads_q
            g = d_ref[h * hd : (h + 1) * hd, :].astype(F32)
            raw = r_ref[h * hd : (h + 1) * hd, :].astype(F32)
            a, b = g[:half], g[half:]
            turned = jnp.concatenate(
                [a * cos_part + b * sin_part, b * cos_part - a * sin_part], axis=0
            )
            rho = lax.rsqrt(jnp.mean(raw * raw, axis=0, keepdims=True) + EPS)
            unit = raw * rho
            prod = turned * unit
            scaled = turned * (qg_ref[...] if is_q else kg_ref[...])
            mean = jnp.mean(scaled * unit, axis=0, keepdims=True)
            done.append(rho * (scaled - unit * mean))
            total = jnp.sum(prod, axis=1, keepdims=True)
            if is_q:
                gain_q = gain_q + total
            else:
                gain_k = gain_k + total
        done.append(d_ref[(heads_q + heads_k) * hd :, :].astype(F32))
        out_ref[0] = jnp.concatenate(done, axis=0).T.astype(BF16)
        lane = lax.broadcasted_iota(jnp.int32, gg_ref.shape, 1)
        gg_ref[...] += jnp.where(lane == 0, gain_q, jnp.where(lane == 1, gain_k, 0.0))

    @pl.when(step == 0)
    def _():
        work(dm_ref, rm_ref)

    @pl.when(step == 1)
    def _():
        work(dt_ref, rt_ref)


def head_back(info, grad_mine, grad_theirs, raw_mine, raw_theirs, cos_part, sin_part, gq, gk, heads):
    cols, tok = grad_mine.shape
    tile = min(512, tok)
    mine = pl.BlockSpec((cols, tile), lambda s, i, info: (0, jnp.where(s == 0, i, tok // tile - 1)))
    theirs = pl.BlockSpec((cols, tile), lambda s, i, info: (0, jnp.where(s == 0, 0, i)))
    tab = lambda a: pl.BlockSpec((a.shape[0], tile), lambda s, i, info: (0, i))
    const = lambda a: pl.BlockSpec(a.shape, lambda s, i, info: (0, 0))
    return pl.pallas_call(
        functools.partial(head_back_kernel, heads),
        grid_spec=pltpu.PrefetchScalarGridSpec(
            num_scalar_prefetch=1,
            grid=(2, tok // tile),
            in_specs=[
                mine,
                theirs,
                mine,
                theirs,
                tab(cos_part),
                tab(sin_part),
                const(gq),
                const(gk),
            ],
            out_specs=[
                pl.BlockSpec(
                    (1, tile, cols), lambda s, i, info: (jnp.bitwise_xor(info[2], s), i, 0)
                ),
                pl.BlockSpec((gq.shape[0], 128), lambda s, i, info: (0, 0)),
            ],
        ),
        out_shape=[shape_of((2, tok, cols), BF16), shape_of((gq.shape[0], 128), F32)],
        compiler_params=settings(2, 24),
        cost_estimate=cost(False),
        name="head_back",
    )(info, grad_mine, grad_theirs, raw_mine, raw_theirs, cos_part, sin_part, gq, gk)


def load_rows(info, mine_ref, got_ref, rows, sems):
    tok = mine_ref.shape[1]
    ctx = info[2]
    here = pl.multiple_of(ctx * tok, tok)
    there = pl.multiple_of((1 - ctx) * tok, tok)
    one = pltpu.make_async_copy(mine_ref, rows.at[:, pl.ds(here, tok)], sems.at[0])
    two = pltpu.make_async_copy(got_ref, rows.at[:, pl.ds(there, tok)], sems.at[1])
    one.start()
    two.start()
    one.wait()
    two.wait()


def keys_with_bias(keys, length):
    hd, slots = keys.shape
    pos = lax.broadcasted_iota(jnp.int32, (hd, slots), 1)
    row = lax.broadcasted_iota(jnp.int32, (hd, slots), 0)
    bias = jnp.where((row == 0) & (pos >= length), NEGATIVE, 0.0)
    return jnp.concatenate([keys.astype(F32), bias], axis=0).T.astype(BF16)


def query_with_one(pair):
    one_row = jnp.where(lax.broadcasted_iota(jnp.int32, pair.shape, 0) == 0, 1.0, 0.0)
    return jnp.concatenate([pair, one_row.astype(BF16)], axis=0)


def causal(scores, width):
    key_pos = lax.broadcasted_iota(jnp.int32, (width, width), 0)
    query_pos = lax.broadcasted_iota(jnp.int32, (width, width), 1)
    allowed = key_pos <= query_pos
    return jnp.where(jnp.concatenate([allowed, allowed], axis=1), scores, NEGATIVE)


def attn_fwd_kernel(
    width, hd, info, mine_ref, got_ref, keep_ref, send_ref, lse_ref, rows, key_rows, sems
):
    head, block = pl.program_id(0), pl.program_id(1)
    heads_k = pl.num_programs(0)
    scale = hd**-0.5 * LOG2E
    length = info[3]
    key_at = pl.multiple_of(heads_k * 2 * hd + head * hd, hd)
    value_at = pl.multiple_of(heads_k * 3 * hd + head * hd, hd)
    query_at = pl.multiple_of(head * 2 * hd, 2 * hd)

    @pl.when((head == 0) & (block == 0))
    def _():
        load_rows(info, mine_ref, got_ref, rows, sems)

    @pl.when(block == 0)
    def _():
        key_rows[...] = keys_with_bias(rows[pl.ds(key_at, hd), :], length)

    start = pl.multiple_of(block * width, width)
    both = rows[pl.ds(query_at, 2 * hd), pl.ds(start, width)]
    query = query_with_one(jnp.concatenate([both[:hd], both[hd:]], axis=1))

    def tile(at, carried, diagonal):
        out, total = carried
        scores = dot(key_rows[pl.ds(at, width), :], query, 1, 0)
        if diagonal:
            scores = causal(scores, width)
        probs = jnp.exp2(scores * scale)
        total = total + jnp.sum(probs, axis=0, keepdims=True)
        out = out + dot(rows[pl.ds(value_at, hd), pl.ds(at, width)], probs.astype(BF16), 1, 0)
        return out, total

    carried = (jnp.zeros((hd, 2 * width), F32), jnp.zeros((1, 2 * width), F32))
    full = jnp.minimum(block, lax.div(length + width - 1, width))
    carried = lax.fori_loop(
        0, full, lambda j, c: tile(pl.multiple_of(j * width, width), c, False), carried
    )
    out, total = tile(start, carried, True)
    out = out * (1.0 / total)
    out = jnp.concatenate([out[:, :width], out[:, width:]], axis=0).T.astype(BF16)
    here = block // 2 == info[2]

    @pl.when(here)
    def _():
        keep_ref[...] = out

    @pl.when(jnp.logical_not(here))
    def _():
        send_ref[...] = out

    log_total = jnp.log2(total)
    lse_ref[0, 0:1, :] = log_total[:, :width]
    lse_ref[0, 1:2, :] = log_total[:, width:]


def keep_block(i, info):
    return jnp.clip(i - 2 * info[2], 0, 1)


def send_block(i, info):
    return jnp.clip(i - 2 * (1 - info[2]), 0, 1)


def attn_fwd(info, mine, got, hd):
    cols, tok = mine.shape
    heads_k = cols // (4 * hd)
    width = tok // 2
    return pl.pallas_call(
        functools.partial(attn_fwd_kernel, width, hd),
        grid_spec=pltpu.PrefetchScalarGridSpec(
            num_scalar_prefetch=1,
            grid=(heads_k, 4),
            in_specs=[ANY, ANY],
            out_specs=[
                pl.BlockSpec((width, 2 * hd), lambda h, i, info: (keep_block(i, info), h)),
                pl.BlockSpec((width, 2 * hd), lambda h, i, info: (send_block(i, info), h)),
                pl.BlockSpec((1, 2, width), lambda h, i, info: (h, 0, i)),
            ],
            scratch_shapes=[
                pltpu.VMEM((cols, 2 * tok), BF16),
                pltpu.VMEM((2 * tok, 2 * hd), BF16),
                pltpu.SemaphoreType.DMA((2,)),
            ],
        ),
        out_shape=[
            shape_of((tok, heads_k * 2 * hd), BF16),
            shape_of((tok, heads_k * 2 * hd), BF16),
            shape_of((heads_k, 2, 2 * tok), F32),
        ],
        compiler_params=settings(2, 60),
        cost_estimate=cost(True),
        name="attn_fwd",
    )(info, mine, got)


def attn_bwd_kernel(
    width,
    hd,
    info,
    mine_ref,
    got_ref,
    ok_ref,
    os_ref,
    gk_ref,
    gs_ref,
    lse_ref,
    keep_ref,
    send_ref,
    rows,
    key_rows,
    value_rows,
    key_sum,
    value_sum,
    sems,
):
    head, block = pl.program_id(0), pl.program_id(1)
    heads_k = pl.num_programs(0)
    scale = hd**-0.5
    length = info[3]
    ctx = info[2]
    tok = keep_ref.shape[1]
    key_at = pl.multiple_of(heads_k * 2 * hd + head * hd, hd)
    value_at = pl.multiple_of(heads_k * 3 * hd + head * hd, hd)
    query_at = pl.multiple_of(head * 2 * hd, 2 * hd)

    @pl.when((head == 0) & (block == 0))
    def _():
        load_rows(info, mine_ref, got_ref, rows, sems)

    @pl.when(block == 0)
    def _():
        key_rows[...] = keys_with_bias(rows[pl.ds(key_at, hd), :], length)
        value_rows[...] = rows[pl.ds(value_at, hd), :].astype(F32).T.astype(BF16)
        key_sum[...] = jnp.zeros_like(key_sum)
        value_sum[...] = jnp.zeros_like(value_sum)

    start = pl.multiple_of(block * width, width)
    here = block // 2 == ctx

    def store_query(value):
        at = pl.ds(pl.multiple_of((block % 2) * width, width), width)

        @pl.when(here)
        def _():
            keep_ref[pl.ds(query_at, 2 * hd), at] = value

        @pl.when(jnp.logical_not(here))
        def _():
            send_ref[pl.ds(query_at, 2 * hd), at] = value

    @pl.when(block * width < length)
    def _():
        both = rows[pl.ds(query_at, 2 * hd), pl.ds(start, width)]
        pair = jnp.concatenate([both[:hd], both[hd:]], axis=1)
        query = query_with_one(pair)
        query_rows = pair.astype(F32).T.astype(BF16)
        grad_wide = jnp.where(here, gk_ref[...].astype(F32), gs_ref[...].astype(F32))
        out_wide = jnp.where(here, ok_ref[...].astype(F32), os_ref[...].astype(F32))
        grad_rows = jnp.concatenate([grad_wide[:, :hd], grad_wide[:, hd:]], axis=0).astype(BF16)
        grad_t = grad_wide.T
        prod = (grad_wide * out_wide).T
        grad = jnp.concatenate([grad_t[:hd], grad_t[hd:]], axis=1).astype(BF16)
        delta = jnp.concatenate(
            [
                jnp.sum(prod[:hd], axis=0, keepdims=True),
                jnp.sum(prod[hd:], axis=0, keepdims=True),
            ],
            axis=1,
        )
        lse = jnp.concatenate([lse_ref[0, 0:1, :], lse_ref[0, 1:2, :]], axis=1)

        def tile(at, query_sum, diagonal):
            scores = dot(key_rows[pl.ds(at, width), :], query, 1, 0)
            if diagonal:
                scores = causal(scores, width)
            probs = jnp.exp2(scores * (scale * LOG2E) - lse)
            grad_probs = dot(value_rows[pl.ds(at, width), :], grad, 1, 0)
            grad_scores = (probs * (grad_probs - delta)).astype(BF16)
            value_sum[pl.ds(at, width), :] += dot(probs.astype(BF16), grad_rows, 1, 0)
            key_sum[pl.ds(at, width), :] += dot(grad_scores, query_rows, 1, 0)
            return query_sum + dot(rows[pl.ds(key_at, hd), pl.ds(at, width)], grad_scores, 1, 0)

        query_sum = lax.fori_loop(
            0,
            block,
            lambda j, s: tile(pl.multiple_of(j * width, width), s, False),
            jnp.zeros((hd, 2 * width), F32),
        )
        query_sum = tile(start, query_sum, True) * scale
        store_query(
            jnp.concatenate([query_sum[:, :width], query_sum[:, width:]], axis=0).astype(BF16)
        )

    @pl.when(block * width >= length)
    def _():
        store_query(jnp.zeros((2 * hd, width), BF16))

    @pl.when(block == 3)
    def _():
        for at, total in ((key_at, key_sum[...] * scale), (value_at, value_sum[...])):
            total = total.T.astype(BF16)
            left, right = total[:, :tok], total[:, tok:]

            @pl.when(ctx == 0)
            def _():
                keep_ref[pl.ds(at, hd), :] = left
                send_ref[pl.ds(at, hd), :] = right

            @pl.when(ctx == 1)
            def _():
                keep_ref[pl.ds(at, hd), :] = right
                send_ref[pl.ds(at, hd), :] = left


def attn_bwd(info, mine, got, out_keep, out_send, grad_keep, grad_send, lse, hd):
    cols, tok = mine.shape
    heads_k = cols // (4 * hd)
    width = tok // 2
    keep = pl.BlockSpec((width, 2 * hd), lambda h, i, info: (keep_block(i, info), h))
    send = pl.BlockSpec((width, 2 * hd), lambda h, i, info: (send_block(i, info), h))
    full = pl.BlockSpec((cols, tok), lambda h, i, info: (0, 0))
    return pl.pallas_call(
        functools.partial(attn_bwd_kernel, width, hd),
        grid_spec=pltpu.PrefetchScalarGridSpec(
            num_scalar_prefetch=1,
            grid=(heads_k, 4),
            in_specs=[
                ANY,
                ANY,
                keep,
                send,
                keep,
                send,
                pl.BlockSpec((1, 2, width), lambda h, i, info: (h, 0, i)),
            ],
            out_specs=[full, full],
            scratch_shapes=[
                pltpu.VMEM((cols, 2 * tok), BF16),
                pltpu.VMEM((2 * tok, 2 * hd), BF16),
                pltpu.VMEM((2 * tok, hd), BF16),
                pltpu.VMEM((2 * tok, hd), F32),
                pltpu.VMEM((2 * tok, hd), F32),
                pltpu.SemaphoreType.DMA((2,)),
            ],
        ),
        out_shape=[shape_of((cols, tok), BF16), shape_of((cols, tok), BF16)],
        compiler_params=settings(2, 60),
        cost_estimate=cost(True),
        name="attn_bwd",
    )(info, mine, got, out_keep, out_send, grad_keep, grad_send, lse)


def load_blocks(plan, pieces, target, sem):
    rows = target.shape[1] // 4

    @pl.when(pl.program_id(0) == 0)
    def _():
        for k, places in enumerate(plan):
            for p, (piece, row) in enumerate(places):
                src = pieces[piece].at[pl.ds(row, rows)]
                pltpu.make_async_copy(src, target.at[k, pl.ds(p * rows, rows)], sem).start()
        pltpu.make_async_copy(target, target, sem).wait()


def out_proj_kernel(plan, count, info, *refs):
    x_ref, a0, a1, b0, b1, gain_ref, r_ref, n_ref, nt_ref, att_ref, w_ref, sem = refs[count:]
    load_blocks(plan, refs, w_ref, sem)
    ctx = info[2]
    total = x_ref[...].astype(F32)
    for j, ref, side in ((0, a0, ctx), (1, a1, ctx), (0, b0, 1 - ctx), (1, b1, 1 - ctx)):
        block = 2 * side + j
        part = ref[...]
        att_ref[block] = part
        total = total + dot(part, w_ref[block], 1, 1)
    rho = lax.rsqrt(jnp.mean(total * total, axis=-1, keepdims=True) + EPS)
    normed = total * rho * gain_ref[...]
    r_ref[...] = total
    n_ref[...] = normed.astype(BF16)
    nt_ref[...] = normed.T.astype(BF16)


def out_proj(info, x, mine, theirs, weights, gain, tile):
    plan, pieces = weights
    tok, width = x.shape
    feats = pieces[0].shape[1]
    rows_of = lambda n: pl.BlockSpec((tile, n), lambda i, info: (i, 0))
    return pl.pallas_call(
        functools.partial(out_proj_kernel, plan, len(pieces)),
        grid_spec=pltpu.PrefetchScalarGridSpec(
            num_scalar_prefetch=1,
            grid=(tok // tile,),
            in_specs=[ANY] * len(pieces)
            + [rows_of(width)]
            + [rows_of(feats)] * 4
            + [pl.BlockSpec((1, width), lambda i, info: (0, 0))],
            out_specs=[
                rows_of(width),
                rows_of(width),
                pl.BlockSpec((width, tile), lambda i, info: (0, i)),
                pl.BlockSpec((4, tile, feats), lambda i, info: (0, i, 0)),
            ],
            scratch_shapes=[pltpu.VMEM((4, width, feats), BF16), pltpu.SemaphoreType.DMA],
        ),
        out_shape=[
            shape_of((tok, width), F32),
            shape_of((tok, width), BF16),
            shape_of((width, tok), BF16),
            shape_of((4, tok, feats), BF16),
        ],
        compiler_params=settings(1, 32),
        cost_estimate=cost(True),
        name="out_proj",
    )(info, *pieces, x, *mine, *theirs, gain)


def norm_two_back_kernel(plan, count, info, *refs):
    g_ref, r_ref, gr_ref, gain_ref, gres_ref, gat_ref, a0, a1, b0, b1, gg_ref, w_ref, sem = refs[count:]
    load_blocks(plan, refs, w_ref, sem)
    ctx = info[2]
    grad, resid = g_ref[...], r_ref[...]
    rho = lax.rsqrt(jnp.mean(resid * resid, axis=-1, keepdims=True) + EPS)
    unit = resid * rho
    scaled = grad * gain_ref[...]
    back = rho * (scaled - unit * jnp.mean(scaled * unit, axis=-1, keepdims=True))
    total = gr_ref[...] + back
    gres_ref[...] = total
    low = total.astype(BF16)
    gat_ref[...] = total.T.astype(BF16)

    @pl.when(pl.program_id(0) == 0)
    def _():
        gg_ref[...] = jnp.zeros_like(gg_ref)

    gg_ref[...] += jnp.sum(grad * unit, axis=0, keepdims=True)
    for j, ref, side in ((0, a0, ctx), (1, a1, ctx), (0, b0, 1 - ctx), (1, b1, 1 - ctx)):
        ref[...] = dot(low, w_ref[2 * side + j], 1, 0).astype(BF16)


def norm_two_back(info, grad, resid, grad_result, gain, weights, tile):
    plan, pieces = weights
    tok, width = grad.shape
    feats = pieces[0].shape[1]
    rows_of = lambda n: pl.BlockSpec((tile, n), lambda i, info: (i, 0))
    row = pl.BlockSpec((1, width), lambda i, info: (0, 0))
    return pl.pallas_call(
        functools.partial(norm_two_back_kernel, plan, len(pieces)),
        grid_spec=pltpu.PrefetchScalarGridSpec(
            num_scalar_prefetch=1,
            grid=(tok // tile,),
            in_specs=[ANY] * len(pieces) + [rows_of(width)] * 3 + [row],
            out_specs=[rows_of(width), pl.BlockSpec((width, tile), lambda i, info: (0, i))]
            + [rows_of(feats)] * 4
            + [row],
            scratch_shapes=[pltpu.VMEM((4, width, feats), BF16), pltpu.SemaphoreType.DMA],
        ),
        out_shape=[shape_of((tok, width), F32), shape_of((width, tok), BF16)]
        + [shape_of((tok, feats), BF16)] * 4
        + [shape_of((1, width), F32)],
        compiler_params=settings(1, 32),
        cost_estimate=cost(True),
        name="norm_two_back",
    )(info, *pieces, grad, resid, grad_result, gain)


def norm_one_back_kernel(plan, count, info, *refs):
    p0, p1, x_ref, gres_ref, gain_ref, *out_refs, gg_ref, w_ref, sem = refs[count:]
    load_blocks(plan, refs, w_ref, sem)
    quarter = x_ref.shape[1] // 4
    grad = dot(p0[0], w_ref[0], 1, 1)
    grad = grad + dot(p1[0], w_ref[1], 1, 1)
    grad = grad + dot(p0[1], w_ref[2], 1, 1)
    grad = grad + dot(p1[1], w_ref[3], 1, 1)
    x = x_ref[...].astype(F32)
    rho = lax.rsqrt(jnp.mean(x * x, axis=-1, keepdims=True) + EPS)
    unit = x * rho
    scaled = grad * gain_ref[...]
    back = rho * (scaled - unit * jnp.mean(scaled * unit, axis=-1, keepdims=True))
    total = (gres_ref[...] + back).astype(BF16)
    for p, mask in enumerate(MASKS):
        at = pl.multiple_of(jnp.bitwise_xor(info[1], mask) * quarter, quarter)
        part = total[:, p * quarter : (p + 1) * quarter]

        for i, out_ref in enumerate(out_refs):

            @pl.when(pl.program_id(0) == i)
            def _():
                out_ref[:, pl.ds(at, quarter)] = part

    @pl.when(pl.program_id(0) == 0)
    def _():
        gg_ref[...] = jnp.zeros_like(gg_ref)

    gg_ref[...] += jnp.sum(grad * unit, axis=0, keepdims=True)


def norm_one_back(info, pairs, weights, x, grad_resid, gain, tile):
    plan, pieces = weights
    tok, width = x.shape
    cols = pieces[0].shape[1]
    rows_of = lambda n: pl.BlockSpec((tile, n), lambda i, info: (i, 0))
    pair = pl.BlockSpec((2, tile, cols), lambda i, info: (0, i, 0))
    row = pl.BlockSpec((1, width), lambda i, info: (0, 0))
    return pl.pallas_call(
        functools.partial(norm_one_back_kernel, plan, len(pieces)),
        grid_spec=pltpu.PrefetchScalarGridSpec(
            num_scalar_prefetch=1,
            grid=(tok // tile,),
            in_specs=[ANY] * len(pieces) + [pair, pair, rows_of(width), rows_of(width), row],
            out_specs=[pl.BlockSpec((tile, width), lambda i, info: (0, 0))] * 4 + [row],
            scratch_shapes=[pltpu.VMEM((4, width, cols), BF16), pltpu.SemaphoreType.DMA],
        ),
        out_shape=[shape_of((tile, width), BF16)] * 4 + [shape_of((1, width), F32)],
        compiler_params=settings(1, 32),
        cost_estimate=cost(True),
        name="norm_one_back",
    )(info, *pieces, *pairs, x, grad_resid, gain)


def weight_copies(plan, pieces, gate_up, down, gate_up_sem, down_sem):
    third = down.shape[1] // 3
    rows = down.shape[0] // 4
    wide, thin = [], []
    for p, chunks in enumerate(plan):
        block = pl.ds(p * rows, rows)
        for j, (piece, row, at) in enumerate(chunks):
            src = pieces[piece].at[pl.ds(row, rows)]
            wide.append(
                pltpu.make_async_copy(
                    src.at[:, pl.ds(at, 2 * third)],
                    gate_up.at[block, pl.ds(j * 2 * third, 2 * third)],
                    gate_up_sem,
                )
            )
            thin.append(
                pltpu.make_async_copy(
                    src.at[:, pl.ds(at + 2 * third, third)],
                    down.at[block, pl.ds(j * third, third)],
                    down_sem,
                )
            )
    return wide, thin


def split_act(act):
    third = act.shape[1] // 6
    part = lambda j: act[:, j * third : (j + 1) * third]
    return [(part(0), part(1)), (part(2), part(3)), (part(4), part(5))]


def ffn_fwd_kernel(tile, plans, last, info, scale, x_ref, in_ref, *rest):
    if last:
        teach_ref, rest = rest[0], rest[1:]
    pieces = []
    for plan in plans:
        count = 1 + max(place[0] for chunks in plan for place in chunks)
        pieces.append(rest[:count])
        rest = rest[count:]
    act_ref, hid_ref = rest[:2]
    if last:
        outa_ref, outb_ref, gres_ref, low_ref, lowt_ref, sq_ref = rest[2:8]
        gate_up, down, total, sems = rest[8:]
    else:
        sum_ref, gate_up, down, total, sems = rest[2:]
    step, part = pl.program_id(0), pl.program_id(1)
    final = len(plans) - 1
    width = x_ref.shape[1]
    quarter = width // 4
    third = down.shape[2] // 3

    def copies(s):
        return weight_copies(
            plans[s], pieces[s], gate_up.at[s], down.at[s], sems.at[s, 0], sems.at[s, 1]
        )

    @pl.when((step == 0) & (part == 0))
    def _():
        for s in range(len(plans)):
            wide, thin = copies(s)
            for copy in wide + thin:
                copy.start()

    for s in range(len(plans)):

        @pl.when((step == s) & (part == 0))
        def _():
            pltpu.make_async_copy(gate_up.at[s], gate_up.at[s], sems.at[s, 0]).wait()
            pltpu.make_async_copy(down.at[s], down.at[s], sems.at[s, 1]).wait()

    rows = pl.ds(pl.multiple_of(part * tile, tile), tile)
    act = dot(x_ref[rows, :], gate_up[step], 1, 0)
    for j, (gate, upper) in enumerate(split_act(act)):
        hid_ref[0, :, j * third : (j + 1) * third] = (gate * sigmoid(gate) * upper).astype(BF16)
    act_ref[0] = act.astype(BF16)
    grown = dot(hid_ref[0], down[step], 1, 1)

    @pl.when(step == 0)
    def _():
        total[rows, :] = in_ref[...] + grown

    @pl.when(step > 0)
    def _():
        total[rows, :] += grown

    @pl.when(step == final)
    def _():
        result = total[rows, :]
        if not last:
            sum_ref[...] = result
            return
        tok = x_ref.shape[0]
        slot = info[2] * tok + part * tile + lax.broadcasted_iota(jnp.int32, (tile, 1), 0)
        valid = jnp.where(slot < info[3], 1.0, 0.0)
        square = jnp.zeros((tile, quarter), F32)
        for p, mask in enumerate(MASKS):
            at = pl.multiple_of(jnp.bitwise_xor(info[1], mask) * quarter, quarter)
            cols = slice(p * quarter, (p + 1) * quarter)
            value = result[:, cols]
            low = value.astype(BF16)

            @pl.when(part < pl.num_programs(1) // 2)
            def _():
                outa_ref[:, pl.ds(at, quarter)] = low

            @pl.when(part >= pl.num_programs(1) // 2)
            def _():
                outb_ref[:, pl.ds(at, quarter)] = low

            error = valid * (value - teach_ref[0, :, pl.ds(at, quarter)].astype(F32))
            square = square + error * error
            grad = error * scale[0]
            gres_ref[:, cols] = grad
            low_ref[:, cols] = grad.astype(BF16)
            lowt_ref[cols, :] = grad.T.astype(BF16)

        @pl.when(part == 0)
        def _():
            sq_ref[...] = jnp.zeros_like(sq_ref)

        sq_ref[...] += jnp.sum(square, axis=0, keepdims=True)


def ffn_fwd(info, scale, x, total, teacher, weights, units, tile):
    tok, width = x.shape
    pieces = [piece for _, group in weights for piece in group]
    count = len(weights)
    last = teacher is not None
    entry = lambda s, i: jnp.where(s == 0, i, tok // tile - 1)
    leave = lambda s, i: jnp.where(s == count - 1, i, 0)
    tiles = lambda n: pl.BlockSpec((tile, n), lambda s, i, info: (leave(s, i), 0))
    slab = lambda n: pl.BlockSpec((1, tile, n), lambda s, i, info: (s, i, 0))
    in_specs = [
        SMEM,
        whole((tok, width)),
        pl.BlockSpec((tile, width), lambda s, i, info: (entry(s, i), 0)),
    ]
    out_specs = [slab(2 * units), slab(units)]
    out_shape = [shape_of((count, tok, 2 * units), BF16), shape_of((count, tok, units), BF16)]
    if last:
        in_specs.append(
            pl.BlockSpec((1, tile, width), lambda s, i, info: (info[0], leave(s, i), 0))
        )
        half = tok // tile // 2
        out_specs += [
            pl.BlockSpec(
                (tile, width), lambda s, i, info: (jnp.minimum(leave(s, i), half - 1), 0)
            ),
            pl.BlockSpec(
                (tile, width), lambda s, i, info: (jnp.maximum(leave(s, i) - half, 0), 0)
            ),
            tiles(width),
            tiles(width),
            pl.BlockSpec((width, tile), lambda s, i, info: (0, leave(s, i))),
            pl.BlockSpec((1, width // 4), lambda s, i, info: (0, 0)),
        ]
        out_shape += [
            shape_of((tok // 2, width), BF16),
            shape_of((tok // 2, width), BF16),
            shape_of((tok, width), F32),
            shape_of((tok, width), BF16),
            shape_of((width, tok), BF16),
            shape_of((1, width // 4), F32),
        ]
    else:
        out_specs.append(tiles(width))
        out_shape.append(shape_of((tok, width), F32))
    return pl.pallas_call(
        functools.partial(ffn_fwd_kernel, tile, [plan for plan, _ in weights], last),
        grid_spec=pltpu.PrefetchScalarGridSpec(
            num_scalar_prefetch=1,
            grid=(count, tok // tile),
            in_specs=in_specs + [ANY] * len(pieces),
            out_specs=out_specs,
            scratch_shapes=[
                pltpu.VMEM((count, width, 2 * units), BF16),
                pltpu.VMEM((count, width, units), BF16),
                pltpu.VMEM((tok, width), F32),
                pltpu.SemaphoreType.DMA((count, 2)),
            ],
        ),
        out_shape=out_shape,
        compiler_params=settings(2, 60),
        cost_estimate=cost(True),
        name="ffn_fwd",
    )(info, scale, x, total, *([teacher] if last else []), *pieces)


def ffn_bwd_kernel(steps, plan, first, low_ref, act_ref, hid_ref, xt_ref, lowt_ref, *rest):
    count = 1 + max(place[0] for chunks in plan for place in chunks)
    pieces, rest = rest[:count], rest[count:]
    if not first:
        in_ref, rest = rest[0], rest[1:]
    out_ref, keep_ref, send_ref, gate_up, down, dact_all, hid_all, sems = rest
    step = pl.program_id(0)
    units = down.shape[1]
    third = units // 3
    tile = low_ref.shape[0]

    @pl.when(step == 0)
    def _():
        wide, thin = weight_copies(plan, pieces, gate_up, down, sems.at[0], sems.at[1])
        for copy in thin + wide:
            copy.start()
        pltpu.make_async_copy(down, down, sems.at[1]).wait()

    @pl.when(step < steps)
    def _():
        rows = pl.ds(pl.multiple_of(step * tile, tile), tile)
        grad_hidden = dot(low_ref[...], down[...], 1, 0)
        for j, (gate, upper) in enumerate(split_act(act_ref[0])):
            grad = grad_hidden[:, j * third : (j + 1) * third]
            gate, upper = gate.astype(F32), upper.astype(F32)
            sig = sigmoid(gate)
            silu = gate * sig
            at = 2 * j * third
            dact_all[rows, at : at + third] = (
                grad * upper * (sig + silu - silu * sig)
            ).astype(BF16)
            dact_all[rows, at + third : at + 2 * third] = (grad * silu).astype(BF16)
        hid_all[rows, :] = hid_ref[0]

        @pl.when(step == 0)
        def _():
            pltpu.make_async_copy(gate_up, gate_up, sems.at[0]).wait()

        grown = dot(dact_all[rows, :], gate_up[...], 1, 1)
        out_ref[...] = grown if first else in_ref[...] + grown

    def weight_rows(target):
        target[:, : 2 * units] = dot(xt_ref[...], dact_all[...], 1, 0).astype(BF16)
        target[:, 2 * units :] = dot(lowt_ref[...], hid_all[...], 1, 0).astype(BF16)

    @pl.when((step >= steps) & (step < steps + 2))
    def _():
        weight_rows(send_ref)

    @pl.when(step >= steps + 2)
    def _():
        weight_rows(keep_ref)


def ffn_bwd(low, saved, weights, total, xt, lowt, tile):
    plan, pieces = weights
    acts, hiddens, block = saved
    tok, width = low.shape
    units = hiddens.shape[2]
    steps = tok // tile
    quarter = width // 4
    first = total is None
    clip = lambda i: jnp.minimum(i, steps - 1)
    rows_of = lambda n: pl.BlockSpec((tile, n), lambda i: (clip(i), 0))
    slab = lambda n: pl.BlockSpec((1, tile, n), lambda i: (block, clip(i), 0))
    feature = lambda i: (jnp.where(i < steps + 2, jnp.maximum(i - steps, 0) + 2, i - steps - 2), 0)
    return pl.pallas_call(
        functools.partial(ffn_bwd_kernel, steps, plan, first),
        grid=(steps + 4,),
        in_specs=[
            rows_of(width),
            slab(2 * units),
            slab(units),
            pl.BlockSpec((quarter, tok), feature),
            pl.BlockSpec((quarter, tok), feature),
        ]
        + [ANY] * len(pieces)
        + ([] if first else [rows_of(width)]),
        out_specs=[
            rows_of(width),
            pl.BlockSpec((quarter, 3 * units), lambda i: (jnp.maximum(i - steps - 2, 0), 0)),
            pl.BlockSpec((quarter, 3 * units), lambda i: (jnp.clip(i - steps, 0, 1), 0)),
        ],
        out_shape=[
            shape_of((tok, width), F32),
            shape_of((width // 2, 3 * units), BF16),
            shape_of((width // 2, 3 * units), BF16),
        ],
        scratch_shapes=[
            pltpu.VMEM((width, 2 * units), BF16),
            pltpu.VMEM((width, units), BF16),
            pltpu.VMEM((tok, 2 * units), BF16),
            pltpu.VMEM((tok, units), BF16),
            pltpu.SemaphoreType.DMA((2,)),
        ],
        input_output_aliases={} if first else {5 + len(pieces): 0},
        compiler_params=settings(1, 60),
        cost_estimate=cost(True),
        name="ffn_bwd",
    )(low, acts, hiddens, xt, lowt, *pieces, *([] if first else [total]))


def turn_chunks(block):
    wide = block.shape[1] * 2 // 9
    thin = wide // 2
    starts = [(2 * wide, wide), (wide, wide), (0, wide)]
    starts += [(3 * wide + 2 * thin, thin), (3 * wide + thin, thin), (3 * wide, thin)]
    return jnp.concatenate([block[:, a : a + n] for a, n in starts], axis=1)


def sum_kernel(turns, *refs):
    total = None
    for ref, turn in zip(refs[:-1], turns):
        value = ref[...].astype(F32)
        value = turn_chunks(value) if turn else value
        total = value if total is None else total + value
    refs[-1][...] = total.astype(refs[-1].dtype)


def summed(terms, turns=None, dtype=BF16):
    rows, cols = terms[0].shape
    spec = pl.BlockSpec((128, cols), lambda i: (i, 0))
    return pl.pallas_call(
        functools.partial(sum_kernel, turns or [False] * len(terms)),
        grid=(rows // 128,),
        in_specs=[spec] * len(terms),
        out_specs=spec,
        out_shape=shape_of((rows, cols), dtype),
        compiler_params=settings(1, 24),
        cost_estimate=cost(False),
        name="summed",
    )(*terms)


def core_sum_kernel(info, left_ref, right_ref, *outs):
    total = (left_ref[...].astype(F32) + right_ref[...].astype(F32)).astype(BF16)
    block = pl.program_id(1)
    place = block // 2 * 2 + jnp.bitwise_xor(block % 2, info[2])
    for i, out in enumerate(outs):

        @pl.when(place == i)
        def _():
            out[...] = total


def core_sum(info, keep, came):
    groups, rows, cols = keep.shape
    spec = pl.BlockSpec((1, rows // 4, cols), lambda g, i, info: (g, i, 0))
    return pl.pallas_call(
        core_sum_kernel,
        grid_spec=pltpu.PrefetchScalarGridSpec(
            num_scalar_prefetch=1,
            grid=(groups, 4),
            in_specs=[spec] * 2,
            out_specs=[pl.BlockSpec((1, rows // 4, cols), lambda g, i, info: (g, 0, 0))] * 4,
        ),
        out_shape=[shape_of((groups, rows // 4, cols), BF16)] * 4,
        compiler_params=settings(2, 24),
        cost_estimate=cost(False),
        name="core_sum",
    )(info, keep, came)


def weight_grad_kernel(nt_ref, back0_ref, back1_ref, gt_ref, att_ref, keep_ref, send_ref):
    cols = back0_ref.shape[2]
    part, block = pl.program_id(0), pl.program_id(1)

    def rows(target, back_ref):
        target[0, :, :cols] = dot(nt_ref[...], back_ref[0], 1, 0).astype(BF16)
        target[0, :, cols:] = dot(gt_ref[...], att_ref[0], 1, 0).astype(BF16)

    for j, back_ref in enumerate((back0_ref, back1_ref)):

        @pl.when((part == 0) & (block % 2 == j))
        def _():
            rows(send_ref, back_ref)

        @pl.when((part == 1) & (block % 2 == j))
        def _():
            rows(keep_ref, back_ref)


def weight_grad(normed_t, backs, grad_t, attended):
    width, tok = normed_t.shape
    cols, feats = backs[0].shape[2], attended.shape[2]
    half = pl.BlockSpec((width // 2, tok), lambda p, k: (1 - p, 0))
    side = pl.BlockSpec((1, tok, cols), lambda p, k: (k // 2, 0, 0))
    shape = (1, width // 2, cols + feats)
    return pl.pallas_call(
        weight_grad_kernel,
        grid=(2, 4),
        in_specs=[half, side, side, half, pl.BlockSpec((1, tok, feats), lambda p, k: (k, 0, 0))],
        out_specs=[
            pl.BlockSpec(shape, lambda p, k: (jnp.where(p == 0, 0, k), 0, 0)),
            pl.BlockSpec(shape, lambda p, k: (jnp.where(p == 0, k, 3), 0, 0)),
        ],
        out_shape=[shape_of((4, width // 2, cols + feats), BF16)] * 2,
        compiler_params=settings(2, 32),
        cost_estimate=cost(True),
        name="weight_grad",
    )(normed_t, *backs, grad_t, attended)


def after(value, *others):
    return lax.optimization_barrier((value,) + others)[0]


def per_device_rows(
    tokens,
    teacher,
    lengths,
    attn_gain,
    q_weight,
    k_weight,
    v_weight,
    q_gain,
    k_gain,
    o_weight,
    ffn_gain,
    gate_weight,
    up_weight,
    down_weight,
):
    z = lax.axis_index("tp")
    ctx = lax.axis_index("ctx")
    fsdp = lax.axis_index("fsdp")
    rows_dev, tok, width = tokens.shape
    quarter = width // 4
    hd = q_gain.shape[0] * 4
    q_cols, k_cols = q_weight.shape[1], k_weight.shape[1]
    proj = q_cols + 2 * k_cols
    heads = (q_cols // hd, k_cols // hd)
    units = gate_weight.shape[1]
    slots = rows_dev * 4 * tok * 2

    def x_swap(v):
        return lax.ppermute(v, "fsdp", X_SWAP)

    def core_swap(v):
        return lax.ppermute(v, "fsdp", CORE_SWAP)

    def y_swap(v):
        return lax.ppermute(v, "ctx", Y_SWAP)

    def z_up(v):
        return lax.ppermute(v, "tp", Z_UP)

    def z_far(v):
        return lax.ppermute(v, "tp", Z_FAR)

    def z_down(v):
        return lax.ppermute(v, "tp", Z_DOWN)

    def natural(v):
        v = jnp.concatenate([v[0:1], v[2:3], v[1:2], v[3:4]], axis=0)
        v = jnp.where(fsdp % 2 == 0, v, jnp.concatenate([v[1:2], v[0:1], v[3:4], v[2:3]], axis=0))
        return jnp.where(fsdp // 2 == 0, v, jnp.concatenate([v[2:4], v[0:2]], axis=0))

    v = {}

    def sync():
        v.update(lax.optimization_barrier(dict(v)))

    length = lax.dynamic_slice_in_dim(lengths, z, 1, 0)
    info = jnp.concatenate([jnp.stack([z, fsdp, ctx]).astype(jnp.int32), length])
    w_proj = join(q_weight, k_weight, v_weight)
    proj_z = [z_up(w_proj), z_far(w_proj), z_down(w_proj)]
    proj_far = x_swap(w_proj)
    proj_core = core_swap(w_proj)
    count_here = jnp.sum(lengths).astype(F32)[None]
    vector = jnp.concatenate([attn_gain, ffn_gain, q_gain, k_gain]).astype(F32)
    vector = jnp.concatenate([vector, count_here, jnp.zeros((640 - 545,), F32)])[None]
    vector = jnp.concatenate([vector, x_swap(vector)], axis=0)
    vector = jnp.concatenate([vector, core_swap(vector)], axis=0)
    w_out, w_ffn, *w_chunks = pack(info, o_weight, gate_weight, up_weight, down_weight)
    pos = (ctx * tok + jnp.arange(tok, dtype=jnp.int32)).astype(F32)
    frequency = THETA ** (-(2.0 * jnp.arange(hd // 2, dtype=F32)) / hd)
    angles = frequency[:, None] * pos[None, :]
    head_gains = natural(vector[:, 2 * quarter : 544])
    v.update(
        info=info,
        w_proj=w_proj,
        proj_far=proj_far,
        proj_core=proj_core,
        proj_z=jnp.concatenate(proj_z, axis=0),
        w_out=w_out,
        w_ffn=w_ffn,
        w_chunks=w_chunks,
        gain_one=vector[:, :quarter].reshape(1, width),
        gain_two=vector[:, quarter : 2 * quarter].reshape(1, width),
        total_count=jnp.sum(vector[:, 544]),
        gain_q=head_gains[:, : hd // 4].reshape(hd, 1),
        gain_k=head_gains[:, hd // 4 :].reshape(hd, 1),
        cos_part=jnp.cos(angles),
        sin_part=jnp.sin(angles),
    )
    sync()
    info = v["info"]

    proj_zfar = x_swap(v["proj_z"])
    out_z = [z_up(v["w_out"]), z_far(v["w_out"]), z_down(v["w_out"])]
    proj_cores = [v["proj_core"], core_swap(v["proj_far"])]
    x_in, normed_one_t = norm_one(info, tokens, v["gain_one"], 256)
    v.update(
        proj_zfar=proj_zfar,
        proj_cores=proj_cores,
        x_in=x_in,
        normed_one_t=normed_one_t,
        out_z=out_z,
    )
    sync()

    proj_cores = v["proj_cores"] + [core_swap(v["proj_z"]), core_swap(v["proj_zfar"])]
    plan_proj = [[(0, 0), (1, 0), (4, 0), (5, 0)]]
    plan_proj += [[(p, k * quarter) for p in (2, 3, 6, 7)] for k in range(3)]
    weights_proj = [v["w_proj"], v["proj_far"], v["proj_z"], v["proj_zfar"]] + proj_cores
    one = [z_up(v["w_chunks"][0]), z_up(v["w_chunks"][3])]
    ffn_far = x_swap(v["w_ffn"])
    tables = [v[name] for name in ("cos_part", "sin_part", "gain_q", "gain_k")]

    def make(block, *then):
        normed_t = after(v["normed_one_t"], *then)
        return project(info, (plan_proj, weights_proj), normed_t, *tables, heads, block)

    theirs = [make(lambda s: 2 * (1 - s[2]))]
    got = [y_swap(theirs[0][0])]
    theirs.append(make(lambda s: 2 * (1 - s[2]) + 1, theirs[0][0]))
    got.append(y_swap(theirs[1][0]))
    mine = [make(lambda s: 2 * s[2], theirs[1][0])]
    mine.append(make(lambda s: 2 * s[2] + 1, mine[0][0]))
    v.update(
        one=one,
        ffn_far=ffn_far,
        weights_proj=weights_proj,
        mine=mine,
        theirs=theirs,
        got0=got[0],
    )
    sync()

    one_far = [x_swap(v["one"][0])]
    three = [z_down(v["w_chunks"][0])]
    own_cores = [core_swap(v["w_ffn"]), core_swap(v["ffn_far"])]
    first = attn_fwd(info, v["mine"][0][0], v["got0"], hd)
    v.update(first=first, got1=got[1], one_far=one_far, three=three, own_cores=own_cores)
    sync()

    arrived = [y_swap(v["first"][1])]
    three = v["three"] + [z_down(v["w_chunks"][1])]
    out_blocks = jnp.concatenate([v["w_out"]] + v["out_z"], axis=0)
    out_far = x_swap(out_blocks)
    one_cores = [core_swap(v["one"][0]), core_swap(v["one_far"][0])]
    second = attn_fwd(info, v["mine"][1][0], v["got1"], hd)
    v.update(
        second=second,
        arrived=arrived,
        three=three,
        out_blocks=out_blocks,
        out_far=out_far,
        one_cores=one_cores,
    )
    sync()

    arrived = v["arrived"] + [y_swap(v["second"][1])]
    three = v["three"] + [z_down(v["w_chunks"][2])]
    one_far = v["one_far"] + [x_swap(v["one"][1][:, :units])]
    weights_out = [v["out_blocks"], v["out_far"]]
    weights_out += [core_swap(v["out_blocks"]), core_swap(v["out_far"])]
    v.update(arrived=arrived, three=three, one_far=one_far, weights_out=weights_out)
    sync()

    plan_out = [[(p, k * quarter) for p in range(4)] for k in range(4)]
    two = [z_up(v["one"][0])]
    three_far = [x_swap(v["three"][0])]
    one_far = v["one_far"] + [y_swap(v["one_far"][0])]
    one_cores = v["one_cores"] + [core_swap(v["one"][1]), core_swap(v["one_far"][1])]
    resid, normed_two, normed_two_t, attended = out_proj(
        info,
        v["x_in"],
        [v["first"][0], v["second"][0]],
        v["arrived"],
        (plan_out, v["weights_out"]),
        v["gain_two"],
        256,
    )
    v.update(
        two=two,
        three_far=three_far,
        one_far=one_far,
        one_cores=one_cores,
        resid=resid,
        normed_two=normed_two,
        normed_two_t=normed_two_t,
        attended=attended,
    )
    sync()

    plan0 = [[(i, 0, j * units) for j in range(3)] for i in range(4)]
    plan_mixed = [[(0, 0, 0), (1, 0, 0), (1, 0, units)], [(i, 0, 0) for i in (2, 3, 4)]]
    plan_mixed += [[(5, 0, 0), (6, 0, 0), (6, 0, units)], [(i, 0, 0) for i in (7, 8, 9)]]
    scale = (slots / v["total_count"])[None]
    weights0 = [v["w_ffn"], v["ffn_far"]] + v["own_cores"]
    c0, cf, c1, cb = v["one_cores"]
    weights1 = v["one"] + v["one_far"] + [c0, c1, cf, cb, core_swap(v["one_far"][2])]
    two = v["two"] + [z_up(v["one"][1])]
    three_far = v["three_far"] + [x_swap(v["three"][1]), y_swap(v["three_far"][0])]
    two_far = [x_swap(v["two"][0])]
    three_cores = [core_swap(v["three"][0])]
    acts_a, hiddens_a, sum_a = ffn_fwd(
        info,
        scale,
        v["normed_two"],
        v["resid"],
        None,
        [(plan0, weights0), (plan_mixed, weights1)],
        units,
        256,
    )
    v.update(
        scale=scale,
        weights0=weights0,
        weights1=weights1,
        two=two,
        three_far=three_far,
        two_far=two_far,
        three_cores=three_cores,
        acts_a=acts_a,
        hiddens_a=hiddens_a,
        sum_a=sum_a,
    )
    sync()

    plan_chunks = [[(3 * p + j, 0, 0) for j in range(3)] for p in range(4)]
    weights3 = v["three"] + v["three_far"] + v["three_cores"]
    weights3 += [core_swap(part) for part in v["three"][1:]]
    weights3 += [core_swap(part) for part in v["three_far"]]
    two_far = v["two_far"] + [x_swap(v["two"][1][:, :units]), y_swap(v["two_far"][0])]
    two_cores = [core_swap(part) for part in v["two"] + v["two_far"]]
    acts_b, hiddens_b, sum_b = ffn_fwd(
        info, v["scale"], v["normed_two"], v["sum_a"], None, [(plan_chunks, weights3)], units, 256
    )
    v.update(
        weights3=weights3,
        two_far=two_far,
        two_cores=two_cores,
        acts_b=acts_b,
        hiddens_b=hiddens_b,
        sum_b=sum_b,
    )
    sync()

    weights2 = v["two"] + v["two_far"] + v["two_cores"]
    weights2 += [core_swap(part) for part in v["two_far"][1:]]
    acts_c, hiddens_c, *results, grad_result, grad_low, grad_low_t, square = ffn_fwd(
        info, v["scale"], v["normed_two"], v["sum_b"], teacher, [(plan_mixed, weights2)], units, 256
    )
    v.update(
        weights2=weights2,
        acts_c=acts_c,
        hiddens_c=hiddens_c,
        results=results,
        grad_result=grad_result,
        grad_low=grad_low,
        grad_low_t=grad_low_t,
        square=square,
    )
    sync()

    def ffn_back(plan, weights, acts, hiddens, block, total):
        return ffn_bwd(
            v["grad_low"],
            (v[acts], v[hiddens], block),
            (plan, v[weights]),
            total,
            v["normed_two_t"],
            v["grad_low_t"],
            256,
        )

    def sum_of(k):
        return [p[0] for p in core_sum(info, v[f"keep{k}"][None], v[f"came{k}"][None])]

    turned = [False, False, True]
    one = [z_up(v["results"][0])]
    total, keep2, send2 = ffn_back(plan_mixed, "weights2", "acts_c", "hiddens_c", 0, None)
    v.update(one=one, total=total, keep2=keep2, send2=send2)
    sync()

    one = v["one"] + [z_up(v["results"][1])]
    came2 = core_swap(v["send2"])
    total, keep1, send1 = ffn_back(plan_mixed, "weights1", "acts_a", "hiddens_a", 1, v["total"])
    v.update(one=one, came2=came2, total=total, keep1=keep1, send1=send1)
    sync()

    out_three = [z_down(v["results"][0])]
    came1 = core_swap(v["send1"])
    sum2 = sum_of(2)
    far_t2 = x_swap(sum2[3])
    total, keep3, send3 = ffn_back(
        plan_chunks, "weights3", "acts_b", "hiddens_b", 0, after(v["total"], sum2[0])
    )
    v.update(
        out_three=out_three,
        came1=came1,
        sum2=sum2,
        far_t2=far_t2,
        total=total,
        keep3=keep3,
        send3=send3,
    )
    sync()

    out_three = v["out_three"] + [z_down(v["results"][1])]
    came3 = core_swap(v["send3"])
    far_h2 = x_swap(v["sum2"][2])
    there2 = y_swap(summed([v["sum2"][1], v["far_t2"]]))
    sum1 = sum_of(1)
    total, keep0, send0 = ffn_back(
        plan0, "weights0", "acts_a", "hiddens_a", 0, after(v["total"], sum1[0])
    )
    v.update(
        out_three=out_three,
        came3=came3,
        far_h2=far_h2,
        there2=there2,
        sum1=sum1,
        total=total,
        keep0=keep0,
        send0=send0,
    )
    sync()

    came0 = core_swap(v["send0"])
    far_t1 = x_swap(v["sum1"][3])
    down2 = z_down(summed([v["sum2"][0], v["far_h2"], v["there2"]], turned))
    sum3 = sum_of(3)
    grad_resid, grad_attn_t, a0, a1, b0, b1, gain_two_sum = norm_two_back(
        info,
        after(v["total"], sum3[0]),
        v["resid"],
        v["grad_result"],
        v["gain_two"],
        (plan_out, v["weights_out"]),
        256,
    )
    grad_got = [y_swap(b0), y_swap(b1)]
    v.update(
        came0=came0,
        far_t1=far_t1,
        down2=down2,
        sum3=sum3,
        grad_resid=grad_resid,
        grad_attn_t=grad_attn_t,
        grad_mine=[a0, a1],
        gain_two_sum=gain_two_sum,
        grad_got0=grad_got[0],
    )
    sync()

    def attn_back(j, grad):
        out, got_ref = v["first" if j == 0 else "second"], v[f"got{j}"]
        return attn_bwd(
            info, v["mine"][j][0], got_ref, out[0], out[1], grad, v[f"grad_got{j}"], out[2], hd
        )

    two = [z_up(v["one"][0])]
    far_h1 = x_swap(v["sum1"][2])
    there1 = y_swap(summed([v["sum1"][1], v["far_t1"]]))
    far_t3 = x_swap(v["sum3"][3])
    sum0 = sum_of(0)
    back0 = attn_back(0, after(v["grad_mine"][0], sum0[0]))
    v.update(
        out_two=two,
        far_h1=far_h1,
        there1=there1,
        far_t3=far_t3,
        sum0=sum0,
        back0=back0,
        grad_got1=grad_got[1],
    )
    sync()

    two = v["out_two"] + [z_up(v["one"][1])]
    heads0 = y_swap(v["back0"][1])
    far_h3 = x_swap(v["sum3"][2])
    far_t0 = x_swap(v["sum0"][3])
    there3 = summed([v["sum3"][1], v["far_t3"]])
    two_down = summed(
        [v["sum1"][0], v["far_h1"], v["there1"], v["down2"]], [False, False, True, False]
    )
    there3_got = y_swap(there3)
    two_down_got = z_down(two_down)
    back1 = attn_back(1, after(v["grad_mine"][1], there3, two_down))
    v.update(
        out_two=two, heads0=heads0, far_h3=far_h3, far_t0=far_t0, there3=there3_got, back1=back1
    )
    sync()

    heads1 = y_swap(v["back1"][1])
    far_h0 = x_swap(v["sum0"][2])
    up3 = z_up(summed([v["sum3"][0], v["far_h3"], v["there3"]], turned))
    tables = [v[name] for name in ("cos_part", "sin_part", "gain_q", "gain_k")]
    head0 = head_back(
        info, v["back0"][0], v["heads0"], v["mine"][0][1], v["theirs"][0][1], *tables, heads
    )
    v.update(heads1=heads1, two_down=two_down_got, head0=head0)
    sync()

    there0 = y_swap(summed([v["sum0"][1], v["far_t0"]]))
    head1 = head_back(
        info, v["back1"][0], v["heads1"], v["mine"][1][1], v["theirs"][1][1], *tables, heads
    )
    *tokens_low, gain_one_sum = norm_one_back(
        info,
        [v["head0"][0], head1[0]],
        (plan_proj, v["weights_proj"]),
        v["x_in"],
        v["grad_resid"],
        v["gain_one"],
        tok // 4,
    )
    v.update(head1=head1, tokens_low=tokens_low, gain_one_sum=gain_one_sum, up3=up3)
    v.update(there0=there0, far_h0=far_h0)
    sync()

    def place(out, parts, k, first):
        row = lax.rem(z - k + 4, 4)
        for j, part in enumerate(parts):
            at = (first + j) * part.shape[0]
            out = lax.dynamic_update_slice(out, part.astype(out.dtype)[None], (row, at, 0))
        return out

    v.update(out_one=v["one"])
    quarters = v["tokens_low"]
    one = [z_up(quarters[0])]
    keep, send = weight_grad(
        v["normed_one_t"], [v["head0"][0], v["head1"][0]], v["grad_attn_t"], v["attended"]
    )
    gain_heads = v["head0"][1] + v["head1"][1]
    vector = jnp.concatenate(
        [
            natural(v["gain_one_sum"].reshape(4, quarter)).reshape(1, width),
            natural(v["gain_two_sum"].reshape(4, quarter)).reshape(1, width),
            gain_heads[:, 0].reshape(1, hd),
            gain_heads[:, 1].reshape(1, hd),
            jnp.sum(v["square"]).reshape(1, 1),
            jnp.zeros((1, 127), F32),
        ],
        axis=1,
    )
    vector = vector + core_swap(vector)
    v.update(one=one, keep=keep, send=send)
    v.update(vector=vector)
    sync()

    one = v["one"] + [z_up(part) for part in v["tokens_low"][1:3]]
    rows = quarter // 2
    flat = lambda a: a.reshape(4 * rows, a.shape[-1])
    sums = [flat(p) for p in core_sum(info, v["keep"], core_swap(v["send"]))]
    far_t = x_swap(sums[3])
    part0 = summed([v["sum0"][0], v["far_h0"], v["there0"]], turned)
    ffn_sum = summed([part0, v["two_down"], v["up3"]], None, F32)
    vector = v["vector"] + x_swap(v["vector"])
    v.update(one=one, sums=sums, far_t=far_t, ffn_sum=ffn_sum, vector=vector)
    sync()

    one = v["one"] + [z_up(v["tokens_low"][3])]
    three = [z_down(v["tokens_low"][0])]
    far_h = x_swap(v["sums"][2])
    there = y_swap(summed([v["sums"][1], v["far_t"]]))
    vector = v["vector"] + y_swap(v["vector"])
    output = jnp.zeros((rows_dev, tok, width), BF16)
    for k, parts in enumerate((v["results"], v["out_one"], v["out_two"], v["out_three"])):
        output = place(output, parts, k, 0)
    v.update(one=one, three=three, far_h=far_h, there=there, vector=vector, output=output)
    sync()

    three = v["three"] + [z_down(v["tokens_low"][1])]
    parts = summed([v["sums"][0], v["far_h"], v["there"]])
    parts = [parts[k * rows : (k + 1) * rows] for k in range(4)]
    parts = [parts[0], z_down(parts[1]), z_far(parts[2]), z_up(parts[3])]
    ffn_other = y_swap(v["ffn_sum"])
    grad = place(jnp.zeros((rows_dev, tok, width), F32), v["tokens_low"], 0, 0)
    v.update(three=three, parts=parts, grad=grad)
    sync()

    three = v["three"] + [z_down(part) for part in v["tokens_low"][2:]]
    attn_sum = summed(v["parts"], None, F32)
    vector = v["vector"] + lax.ppermute(v["vector"], "tp", Z_NEAR)
    grad = place(v["grad"], v["one"], 1, 0)
    v.update(three=three, attn_sum=attn_sum, vector=vector, grad=grad, ffn_other=ffn_other)
    sync()

    two = [z_up(part) for part in v["one"][:2]]
    attn_other = y_swap(v["attn_sum"])
    vector = v["vector"] + lax.ppermute(v["vector"], "tp", Z_FAR)
    grad = place(v["grad"], v["three"], 3, 0)
    v.update(two=two, vector=vector, grad=grad, attn_other=attn_other)
    sync()

    two = [z_up(part) for part in v["one"][2:]]
    tokens_grad = place(place(v["grad"], v["two"], 2, 0), two, 2, 2)
    output = v["output"]
    sums = v["vector"][0]

    def finish(own, other):
        return jnp.concatenate(
            [jnp.where(ctx == 0, own, other), jnp.where(ctx == 0, other, own)], axis=0
        )

    ffn_grad = finish(v["ffn_sum"], turn_chunks(v["ffn_other"]))
    attn_grad = finish(v["attn_sum"], v["attn_other"])
    teacher_loss = sums[2 * width + 2 * hd] / (v["total_count"] * width)

    def own_part(at, size):
        return lax.dynamic_slice_in_dim(sums, at + fsdp * (size // 4), size // 4, 0)

    third = units // 3

    def columns(first):
        starts = [first(j) for j in range(3)]
        parts = [ffn_grad[:, s : s + third] for s in starts]
        return jnp.concatenate(
            [jnp.where(ctx == 0, parts[0], parts[2]), parts[1], jnp.where(ctx == 0, parts[2], parts[0])],
            axis=1,
        )

    return (
        output,
        teacher_loss,
        tokens_grad,
        own_part(0, width),
        attn_grad[:, :q_cols],
        attn_grad[:, q_cols : q_cols + k_cols],
        attn_grad[:, q_cols + k_cols : proj],
        own_part(2 * width, hd),
        own_part(2 * width + hd, hd),
        attn_grad[:, proj:].T,
        own_part(width, width),
        columns(lambda j: 2 * j * third),
        columns(lambda j: (2 * j + 1) * third),
        columns(lambda j: 2 * units + j * third).T,
    )


def solution(mesh):
    return jax.shard_map(
        per_device_rows if fits(mesh) else per_device_any,
        mesh=mesh,
        in_specs=(
            P("fsdp", "ctx", None),
            P("fsdp", "ctx", None),
            P("fsdp"),
            P("fsdp"),
            P("fsdp", "tp"),
            P("fsdp", "tp"),
            P("fsdp", "tp"),
            P("fsdp"),
            P("fsdp"),
            P("tp", "fsdp"),
            P("fsdp"),
            P("fsdp", "tp"),
            P("fsdp", "tp"),
            P("tp", "fsdp"),
        ),
        out_specs=(
            P("fsdp", "ctx", None),
            P(),
            P("fsdp", "ctx", None),
            P("fsdp"),
            P("fsdp", "tp"),
            P("fsdp", "tp"),
            P("fsdp", "tp"),
            P("fsdp"),
            P("fsdp"),
            P("tp", "fsdp"),
            P("fsdp"),
            P("fsdp", "tp"),
            P("fsdp", "tp"),
            P("tp", "fsdp"),
        ),
        check_vma=False,
    )
```

```python
import functools
import math

import jax
import jax.numpy as jnp
from jax import lax
from jax.experimental import pallas as pl
from jax.experimental.pallas import tpu as pltpu
from jax.sharding import PartitionSpec as P

EPS = 1e-05
THETA = 1000000.0
NEGATIVE = -1e30


def rms_scale(field_in, gain_vec):
    return (
        field_in * lax.rsqrt(jnp.mean(field_in * field_in, axis=-1, keepdims=True) + EPS) * gain_vec
    )


def rotate(field_in, positions):
    half_dim = field_in.shape[-1] // 2
    frequency = THETA ** (-(2.0 * jnp.arange(half_dim, dtype=jnp.float32)) / field_in.shape[-1])
    angles = positions[:, None] * frequency[None, :]
    cos_part = jnp.cos(angles)[:, None, :]
    sin_part = jnp.sin(angles)[:, None, :]
    lower_half = field_in[..., :half_dim]
    upper_half = field_in[..., half_dim:]
    return jnp.concatenate(
        [
            lower_half * cos_part - upper_half * sin_part,
            upper_half * cos_part + lower_half * sin_part,
        ],
        axis=-1,
    )


def linear(left_mat, right_mat):
    return jnp.dot(left_mat, right_mat, preferred_element_type=jnp.float32)


def linear_left(left_mat, right_mat):
    return lax.dot_general(
        left_mat, right_mat, (((0,), (0,)), ((), ())), preferred_element_type=jnp.float32
    )


def linear_right(left_mat, right_mat):
    return lax.dot_general(
        left_mat, right_mat, (((1,), (1,)), ((), ())), preferred_element_type=jnp.float32
    )


def swiglu(gate_act, up_act):
    return jax.nn.silu(gate_act) * up_act


def per_device_any(
    tokens,
    teacher,
    lengths,
    attn_gain,
    q_weight,
    k_weight,
    v_weight,
    q_gain,
    k_gain,
    o_weight,
    ffn_gain,
    gate_weight,
    up_weight,
    down_weight,
):
    (
        gain_one,
        w_query,
        w_key,
        w_value,
        gain_query,
        gain_key,
        w_output,
        gain_two,
        w_gate,
        w_upper,
        w_down,
    ) = (
        lax.all_gather(attn_gain, "fsdp", axis=0, tiled=True),
        lax.all_gather(q_weight, "fsdp", axis=0, tiled=True),
        lax.all_gather(k_weight, "fsdp", axis=0, tiled=True),
        lax.all_gather(v_weight, "fsdp", axis=0, tiled=True),
        lax.all_gather(q_gain, "fsdp", axis=0, tiled=True),
        lax.all_gather(k_gain, "fsdp", axis=0, tiled=True),
        lax.all_gather(o_weight, "fsdp", axis=1, tiled=True),
        lax.all_gather(ffn_gain, "fsdp", axis=0, tiled=True),
        lax.all_gather(gate_weight, "fsdp", axis=0, tiled=True),
        lax.all_gather(up_weight, "fsdp", axis=0, tiled=True),
        lax.all_gather(down_weight, "fsdp", axis=1, tiled=True),
    )
    rows_dev, block_len, model_width = tokens.shape
    count_tok = rows_dev * block_len
    head_dim = gain_query.shape[0]
    q_heads = w_query.shape[1] // head_dim
    kv_heads = w_key.shape[1] // head_dim
    group_size = q_heads // kv_heads
    score_scale = head_dim ** (-0.5)
    row_len = block_len * lax.axis_size("ctx")
    key_block = math.gcd(row_len, 512)
    block_start = lax.axis_index("ctx") * block_len
    tiles_used = (block_start + block_len + key_block - 1) // key_block
    slot_pos = block_start + jnp.arange(block_len, dtype=jnp.int32)
    positions = slot_pos.astype(jnp.float32)
    valid = (slot_pos[None, :] < lengths[:, None]).astype(jnp.float32)
    slots = count_tok * lax.axis_size("fsdp") * lax.axis_size("ctx")
    gain_two_f = gain_two.astype(jnp.float32)
    gain_one_f = gain_one.astype(jnp.float32)
    inputs = tokens.astype(jnp.float32)
    normed_one, back_one = jax.vjp(rms_scale, inputs, gain_one_f)
    normed_low = normed_one.astype(jnp.bfloat16).reshape(count_tok, model_width)
    query_raw = linear(normed_low, w_query)
    key_raw = linear(normed_low, w_key)
    value_raw = linear(normed_low, w_value)

    def heads_post(raw_heads, gain_vec):
        shaped = raw_heads.reshape(rows_dev, block_len, -1, head_dim)
        return rotate(rms_scale(shaped, gain_vec), positions)

    query_rot, query_back = jax.vjp(heads_post, query_raw, gain_query.astype(jnp.float32))
    key_rot, key_back = jax.vjp(heads_post, key_raw, gain_key.astype(jnp.float32))
    queries = query_rot.astype(jnp.bfloat16).reshape(
        rows_dev, block_len, kv_heads, group_size, head_dim
    )
    key_rows = key_rot.astype(jnp.bfloat16).reshape(rows_dev, block_len, kv_heads * head_dim)
    values = value_raw.astype(jnp.bfloat16).reshape(rows_dev, block_len, kv_heads * head_dim)
    keys_all, values_all = (
        lax.all_gather(key_rows, "ctx", axis=1, tiled=True),
        lax.all_gather(values, "ctx", axis=1, tiled=True),
    )

    def key_tile(tile_index):
        tile_start = tile_index * key_block
        key_pos = tile_start + jnp.arange(key_block, dtype=jnp.int32)
        key_part = lax.dynamic_slice_in_dim(keys_all, tile_start, key_block, 1).reshape(
            rows_dev, key_block, kv_heads, head_dim
        )
        value_part = lax.dynamic_slice_in_dim(values_all, tile_start, key_block, 1).reshape(
            rows_dev, key_block, kv_heads, head_dim
        )
        scores = (
            jnp.einsum("rqhgd,rkhd->rhgqk", queries, key_part, preferred_element_type=jnp.float32)
            * score_scale
        )
        allowed = (key_pos[None, None, :] <= slot_pos[None, :, None]) & (
            key_pos[None, None, :] < lengths[:, None, None]
        )
        return (tile_start, scores, allowed[:, None, None], key_part, value_part)

    stat_shape = (rows_dev, kv_heads, group_size, block_len)

    def stats_step(tile_index, carried):
        running_max, running_sum = carried
        tile_start, scores, allowed, key_part, value_part = key_tile(tile_index)
        masked = jnp.where(allowed, scores, NEGATIVE)
        new_max = jnp.maximum(running_max, jnp.max(masked, axis=-1))
        terms = jnp.where(allowed, jnp.exp(masked - new_max[..., None]), 0.0)
        return (new_max, running_sum * jnp.exp(running_max - new_max) + jnp.sum(terms, axis=-1))

    running_max, running_sum = lax.fori_loop(
        0,
        tiles_used,
        stats_step,
        (jnp.full(stat_shape, NEGATIVE, jnp.float32), jnp.zeros(stat_shape, jnp.float32)),
    )
    log_total = running_max + jnp.log(running_sum)
    out_shape = (rows_dev, block_len, kv_heads, group_size, head_dim)

    def value_step(tile_index, carried):
        rounded_out, exact_out = carried
        tile_start, scores, allowed, key_part, value_part = key_tile(tile_index)
        tile_probs = jnp.where(allowed, jnp.exp(scores - log_total[..., None]), 0.0)
        rounded_out = rounded_out + jnp.einsum(
            "rhgqk,rkhd->rqhgd",
            tile_probs.astype(jnp.bfloat16),
            value_part,
            preferred_element_type=jnp.float32,
        )
        exact_out = exact_out + jnp.einsum(
            "rhgqk,rkhd->rqhgd", tile_probs, value_part.astype(jnp.float32)
        )
        return (rounded_out, exact_out)

    rounded_out, exact_out = lax.fori_loop(
        0,
        tiles_used,
        value_step,
        (jnp.zeros(out_shape, jnp.float32), jnp.zeros(out_shape, jnp.float32)),
    )
    attended = rounded_out.astype(jnp.bfloat16).reshape(count_tok, q_heads * head_dim)
    attn_total = lax.psum(linear(attended, w_output), "tp")
    resid = inputs + attn_total.reshape(rows_dev, block_len, model_width)
    normed_two, back_two = jax.vjp(rms_scale, resid, gain_two_f)
    normed_second = normed_two.astype(jnp.bfloat16).reshape(count_tok, model_width)
    gate_act = linear(normed_second, w_gate)
    up_act = linear(normed_second, w_upper)
    hidden_full, back_glu = jax.vjp(swiglu, gate_act, up_act)
    hidden = hidden_full.astype(jnp.bfloat16)
    ffn_total = lax.psum(linear(hidden, w_down), "tp")
    result = resid + ffn_total.reshape(rows_dev, block_len, model_width)
    error_value = result - teacher.astype(jnp.float32)
    valid_col = valid[..., None]
    total_square, total_count = lax.psum(
        (jnp.sum(valid_col * error_value * error_value), jnp.sum(valid)), ("fsdp", "ctx")
    )
    teacher_loss = total_square / (total_count * model_width)
    grad_result = valid_col * error_value * (slots / total_count)
    grad_low = grad_result.astype(jnp.bfloat16).reshape(count_tok, model_width)
    grad_down = linear_left(hidden, grad_low)
    grad_hidden = linear_right(grad_low, w_down)
    grad_gate_full, grad_up_full = back_glu(grad_hidden)
    grad_gate = grad_gate_full.astype(jnp.bfloat16)
    grad_up = grad_up_full.astype(jnp.bfloat16)
    grad_wgate = linear_left(normed_second, grad_gate)
    grad_wup = linear_left(normed_second, grad_up)
    normed_two_part = linear_right(grad_gate, w_gate) + linear_right(grad_up, w_upper)
    grad_normed_two = lax.psum(normed_two_part, "tp")
    grad_resid_norm, grad_gain_two = back_two(
        grad_normed_two.reshape(rows_dev, block_len, model_width)
    )
    grad_resid = grad_result + grad_resid_norm
    grad_attn_low = grad_resid.astype(jnp.bfloat16).reshape(count_tok, model_width)
    grad_woutput = linear_left(attended, grad_attn_low)
    grad_attended = linear_right(grad_attn_low, w_output).astype(jnp.bfloat16).reshape(out_shape)
    delta = jnp.einsum("rqhgd,rqhgd->rhgq", grad_attended.astype(jnp.float32), exact_out)
    full_shape = (rows_dev, row_len, kv_heads * head_dim)

    def grad_step(tile_index, carried):
        grad_queries, grad_keys, grad_values = carried
        tile_start, scores, allowed, key_part, value_part = key_tile(tile_index)
        tile_probs = jnp.where(allowed, jnp.exp(scores - log_total[..., None]), 0.0)
        grad_probs = jnp.einsum(
            "rqhgd,rkhd->rhgqk", grad_attended, value_part, preferred_element_type=jnp.float32
        )
        grad_scores = (tile_probs * (grad_probs - delta[..., None])).astype(jnp.bfloat16)
        grad_queries = (
            grad_queries
            + jnp.einsum(
                "rhgqk,rkhd->rqhgd", grad_scores, key_part, preferred_element_type=jnp.float32
            )
            * score_scale
        )
        key_term = (
            jnp.einsum(
                "rhgqk,rqhgd->rkhd", grad_scores, queries, preferred_element_type=jnp.float32
            )
            * score_scale
        )
        value_term = jnp.einsum(
            "rhgqk,rqhgd->rkhd",
            tile_probs.astype(jnp.bfloat16),
            grad_attended,
            preferred_element_type=jnp.float32,
        )
        grad_keys = lax.dynamic_update_slice_in_dim(
            grad_keys, key_term.reshape(rows_dev, key_block, kv_heads * head_dim), tile_start, 1
        )
        grad_values = lax.dynamic_update_slice_in_dim(
            grad_values, value_term.reshape(rows_dev, key_block, kv_heads * head_dim), tile_start, 1
        )
        return (grad_queries, grad_keys, grad_values)

    grad_queries, grad_keys, grad_values = lax.fori_loop(
        0,
        tiles_used,
        grad_step,
        (
            jnp.zeros(out_shape, jnp.float32),
            jnp.zeros(full_shape, jnp.float32),
            jnp.zeros(full_shape, jnp.float32),
        ),
    )
    key_grad, value_grad = (
        lax.psum_scatter(grad_keys, "ctx", scatter_dimension=1, tiled=True),
        lax.psum_scatter(grad_values, "ctx", scatter_dimension=1, tiled=True),
    )
    grad_query_raw, grad_gain_query = query_back(
        grad_queries.reshape(rows_dev, block_len, q_heads, head_dim)
    )
    grad_key_raw, grad_gain_key = key_back(
        key_grad.reshape(rows_dev, block_len, kv_heads, head_dim)
    )
    query_low = grad_query_raw.astype(jnp.bfloat16)
    key_low = grad_key_raw.astype(jnp.bfloat16)
    value_low = value_grad.reshape(count_tok, kv_heads * head_dim).astype(jnp.bfloat16)
    grad_wquery = linear_left(normed_low, query_low)
    grad_wkey = linear_left(normed_low, key_low)
    grad_wvalue = linear_left(normed_low, value_low)
    normed_part = (
        linear_right(query_low, w_query)
        + linear_right(key_low, w_key)
        + linear_right(value_low, w_value)
    )
    grad_normed_one, grad_gain_query, grad_gain_key = lax.psum(
        (normed_part, grad_gain_query, grad_gain_key), "tp"
    )
    grad_input_norm, grad_gain_one = back_one(
        grad_normed_one.reshape(rows_dev, block_len, model_width)
    )
    tokens_grad = grad_resid + grad_input_norm
    partials = (
        grad_gain_one,
        grad_wquery,
        grad_wkey,
        grad_wvalue,
        grad_gain_query,
        grad_gain_key,
        grad_woutput,
        grad_gain_two,
        grad_wgate,
        grad_wup,
        grad_down,
    )
    pieces = (
        lax.psum_scatter(partials[0], ("fsdp", "ctx"), scatter_dimension=0, tiled=True),
        lax.psum_scatter(partials[1], ("fsdp", "ctx"), scatter_dimension=0, tiled=True),
        lax.psum_scatter(partials[2], ("fsdp", "ctx"), scatter_dimension=0, tiled=True),
        lax.psum_scatter(partials[3], ("fsdp", "ctx"), scatter_dimension=0, tiled=True),
        lax.psum_scatter(partials[4], ("fsdp", "ctx"), scatter_dimension=0, tiled=True),
        lax.psum_scatter(partials[5], ("fsdp", "ctx"), scatter_dimension=0, tiled=True),
        lax.psum_scatter(partials[6], ("fsdp", "ctx"), scatter_dimension=1, tiled=True),
        lax.psum_scatter(partials[7], ("fsdp", "ctx"), scatter_dimension=0, tiled=True),
        lax.psum_scatter(partials[8], ("fsdp", "ctx"), scatter_dimension=0, tiled=True),
        lax.psum_scatter(partials[9], ("fsdp", "ctx"), scatter_dimension=0, tiled=True),
        lax.psum_scatter(partials[10], ("fsdp", "ctx"), scatter_dimension=1, tiled=True),
    )
    summed = (
        lax.all_gather(pieces[0], "ctx", axis=0, tiled=True),
        lax.all_gather(pieces[1], "ctx", axis=0, tiled=True),
        lax.all_gather(pieces[2], "ctx", axis=0, tiled=True),
        lax.all_gather(pieces[3], "ctx", axis=0, tiled=True),
        lax.all_gather(pieces[4], "ctx", axis=0, tiled=True),
        lax.all_gather(pieces[5], "ctx", axis=0, tiled=True),
        lax.all_gather(pieces[6], "ctx", axis=1, tiled=True),
        lax.all_gather(pieces[7], "ctx", axis=0, tiled=True),
        lax.all_gather(pieces[8], "ctx", axis=0, tiled=True),
        lax.all_gather(pieces[9], "ctx", axis=0, tiled=True),
        lax.all_gather(pieces[10], "ctx", axis=1, tiled=True),
    )
    return (
        result.astype(jnp.bfloat16),
        teacher_loss,
        tokens_grad,
        summed[0],
        summed[1],
        summed[2],
        summed[3],
        summed[4],
        summed[5],
        summed[6],
        summed[7],
        summed[8],
        summed[9],
        summed[10],
    )


BF16 = jnp.bfloat16
F32 = jnp.float32
LOG2E = math.log2(math.e)
X_SWAP = [(0, 2), (2, 0), (1, 3), (3, 1)]
CORE_SWAP = [(0, 1), (1, 0), (2, 3), (3, 2)]
Y_SWAP = [(0, 1), (1, 0)]
Z_UP = [(0, 1), (1, 2), (2, 3), (3, 0)]
Z_DOWN = [(0, 3), (1, 0), (2, 1), (3, 2)]
Z_NEAR = [(0, 1), (1, 0), (2, 3), (3, 2)]
Z_FAR = [(0, 2), (2, 0), (1, 3), (3, 1)]
MASKS = (0, 2, 1, 3)
ANY = pl.BlockSpec(memory_space=pl.ANY)
SMEM = pl.BlockSpec(memory_space=pltpu.SMEM)


def fits(mesh):
    return dict(mesh.shape) == {"fsdp": 4, "ctx": 2, "tp": 4}


def dot(left, right, left_dim, right_dim):
    return lax.dot_general(
        left, right, (((left_dim,), (right_dim,)), ((), ())), preferred_element_type=F32
    )


def sigmoid(v):
    return 0.5 * jnp.tanh(0.5 * v) + 0.5


def whole(shape):
    zeros = (0,) * len(shape)
    return pl.BlockSpec(shape, lambda *_: zeros, pipeline_mode=pl.Buffered(1))


def settings(dims, mib):
    return pltpu.CompilerParams(
        dimension_semantics=("arbitrary",) * dims, vmem_limit_bytes=mib << 20
    )


def shape_of(shape, dtype):
    return jax.ShapeDtypeStruct(shape, dtype)


def cost(large):
    size = 1 << 42 if large else 1 << 10
    return pl.CostEstimate(flops=size, bytes_accessed=size >> 12, transcendentals=0)


def pack_kernel(info, o_in, g_in, u_in, d_in, *refs):
    out_ref, ffn_ref, *chunk_refs, others_ref, o_ref, g_ref, u_ref, d_ref, sems = refs
    ctx = info[2]
    pairs = ((o_in, o_ref), (g_in, g_ref), (u_in, u_ref), (d_in, d_ref))
    copies = [pltpu.make_async_copy(a, b, sems.at[i]) for i, (a, b) in enumerate(pairs)]
    for copy in copies:
        copy.start()
    for copy in copies:
        copy.wait()
    out_ref[...] = o_ref[...].astype(F32).T.astype(BF16)
    third = g_ref.shape[1] // 3
    for j in range(3):
        at = pl.multiple_of(jnp.where(ctx == 0, j, 2 - j) * third, third)
        parts = [
            g_ref[:, pl.ds(at, third)],
            u_ref[:, pl.ds(at, third)],
            d_ref[pl.ds(at, third), :].astype(F32).T.astype(BF16),
        ]
        for i, part in enumerate(parts):
            chunk_refs[j][:, i * third : (i + 1) * third] = part
            if j:
                others_ref[:, (3 * j - 3 + i) * third : (3 * j - 2 + i) * third] = part
            ffn_ref[:, (3 * j + i) * third : (3 * j + i + 1) * third] = part


def pack(info, o, g, u, d):
    rows, units = g.shape
    feats = o.shape[0]
    widths = (feats, 3 * units, units, units, units, 2 * units)
    return pl.pallas_call(
        pack_kernel,
        in_specs=[SMEM] + [ANY] * 4,
        out_specs=[pl.BlockSpec(memory_space=pltpu.VMEM)] * 6,
        out_shape=[shape_of((rows, n), BF16) for n in widths],
        scratch_shapes=[pltpu.VMEM(a.shape, BF16) for a in (o, g, u, d)]
        + [pltpu.SemaphoreType.DMA((4,))],
        compiler_params=pltpu.CompilerParams(vmem_limit_bytes=24 << 20),
        cost_estimate=cost(False),
        name="pack",
    )(info, o, g, u, d)


def join_kernel(q_ref, k_ref, v_ref, out_ref):
    at = 0
    for ref in (q_ref, k_ref, v_ref):
        out_ref[:, at : at + ref.shape[1]] = ref[...]
        at += ref.shape[1]


def join(q, k, v):
    return pl.pallas_call(
        join_kernel,
        out_shape=shape_of((q.shape[0], q.shape[1] + k.shape[1] + v.shape[1]), BF16),
        compiler_params=pltpu.CompilerParams(vmem_limit_bytes=8 << 20),
        cost_estimate=cost(False),
        name="join",
    )(q, k, v)


def norm_one_kernel(info, tok_ref, gain_ref, x_ref, nt_ref, x32):
    quarter = x_ref.shape[1] // 4
    for p, mask in enumerate(MASKS):
        at = pl.multiple_of(jnp.bitwise_xor(info[1], mask) * quarter, quarter)
        part = tok_ref[0, :, pl.ds(at, quarter)]
        x_ref[:, p * quarter : (p + 1) * quarter] = part
        x32[:, p * quarter : (p + 1) * quarter] = part.astype(F32)
    x = x32[...]
    rho = lax.rsqrt(jnp.mean(x * x, axis=-1, keepdims=True) + EPS)
    nt_ref[...] = (x * rho * gain_ref[...]).T.astype(BF16)


def norm_one(info, tokens, gain, tile):
    _, tok, width = tokens.shape
    return pl.pallas_call(
        norm_one_kernel,
        grid_spec=pltpu.PrefetchScalarGridSpec(
            num_scalar_prefetch=1,
            grid=(tok // tile,),
            in_specs=[
                pl.BlockSpec((1, tile, width), lambda i, info: (info[0], i, 0)),
                pl.BlockSpec((1, width), lambda i, info: (0, 0)),
            ],
            out_specs=[
                pl.BlockSpec((tile, width), lambda i, info: (i, 0)),
                pl.BlockSpec((width, tile), lambda i, info: (0, i)),
            ],
            scratch_shapes=[pltpu.VMEM((tile, width), F32)],
        ),
        out_shape=[shape_of((tok, width), BF16), shape_of((width, tok), BF16)],
        compiler_params=settings(1, 24),
        cost_estimate=cost(False),
        name="norm_one",
    )(info, tokens, gain)


def proj_kernel(heads, block, plan, count, info, *refs):
    nt_ref, cos_ref, sin_ref, qg_ref, kg_ref, rot_ref, raw_ref, w_ref, sem = refs[count:]
    rows = w_ref.shape[0] // 4

    @pl.when(pl.program_id(0) == 0)
    def _():
        for k in range(4):

            @pl.when(block(info) == k)
            def _():
                for p, (piece, row) in enumerate(plan[k]):
                    src = refs[piece].at[pl.ds(row, rows)]
                    pltpu.make_async_copy(src, w_ref.at[pl.ds(p * rows, rows)], sem).start()

        pltpu.make_async_copy(w_ref, w_ref, sem).wait()

    hd = qg_ref.shape[0]
    half = hd // 2
    raw = dot(w_ref[...], nt_ref[...], 0, 0)
    cos_part, sin_part = cos_ref[...], sin_ref[...]
    heads_q, heads_k = heads
    raw_ref[...] = raw.astype(BF16)
    for h in range(heads_q + heads_k):
        v = raw[h * hd : (h + 1) * hd]
        rho = lax.rsqrt(jnp.mean(v * v, axis=0, keepdims=True) + EPS)
        v = v * rho * (qg_ref[...] if h < heads_q else kg_ref[...])
        a, b = v[:half], v[half:]
        rot_ref[h * hd : h * hd + half, :] = (a * cos_part - b * sin_part).astype(BF16)
        rot_ref[h * hd + half : (h + 1) * hd, :] = (b * cos_part + a * sin_part).astype(BF16)
    at = (heads_q + heads_k) * hd
    rot_ref[at:, :] = raw[at:].astype(BF16)


def project(info, weights, normed_t, cos_part, sin_part, gain_q, gain_k, heads, block):
    plan, pieces = weights
    width, tok = normed_t.shape
    cols = pieces[0].shape[1]
    tile = min(512, tok)
    const = lambda a: pl.BlockSpec(a.shape, lambda i, info: (0, 0))
    tab = lambda a: pl.BlockSpec((a.shape[0], tile), lambda i, info: (0, i))
    return pl.pallas_call(
        functools.partial(proj_kernel, heads, block, plan, len(pieces)),
        grid_spec=pltpu.PrefetchScalarGridSpec(
            num_scalar_prefetch=1,
            grid=(tok // tile,),
            in_specs=[ANY] * len(pieces)
            + [tab(normed_t), tab(cos_part), tab(sin_part), const(gain_q), const(gain_k)],
            out_specs=[pl.BlockSpec((cols, tile), lambda i, info: (0, i))] * 2,
            scratch_shapes=[pltpu.VMEM((width, cols), BF16), pltpu.SemaphoreType.DMA],
        ),
        out_shape=[shape_of((cols, tok), BF16), shape_of((cols, tok), BF16)],
        compiler_params=settings(1, 24),
        cost_estimate=cost(False),
        name="project",
    )(info, *pieces, normed_t, cos_part, sin_part, gain_q, gain_k)


def head_back_kernel(
    heads, info, dm_ref, dt_ref, rm_ref, rt_ref, cos_ref, sin_ref, qg_ref, kg_ref, out_ref, gg_ref
):
    step, part = pl.program_id(0), pl.program_id(1)
    hd = qg_ref.shape[0]
    half = hd // 2
    heads_q, heads_k = heads
    cos_part, sin_part = cos_ref[...], sin_ref[...]
    tile = cos_part.shape[1]

    @pl.when((step == 0) & (part == 0))
    def _():
        gg_ref[...] = jnp.zeros_like(gg_ref)

    def work(d_ref, r_ref):
        gain_q = jnp.zeros((hd, 1), F32)
        gain_k = jnp.zeros((hd, 1), F32)
        done = []
        for h in range(heads_q + heads_k):
            is_q = h < heads_q
            g = d_ref[h * hd : (h + 1) * hd, :].astype(F32)
            raw = r_ref[h * hd : (h + 1) * hd, :].astype(F32)
            a, b = g[:half], g[half:]
            turned = jnp.concatenate(
                [a * cos_part + b * sin_part, b * cos_part - a * sin_part], axis=0
            )
            rho = lax.rsqrt(jnp.mean(raw * raw, axis=0, keepdims=True) + EPS)
            unit = raw * rho
            prod = turned * unit
            scaled = turned * (qg_ref[...] if is_q else kg_ref[...])
            mean = jnp.mean(scaled * unit, axis=0, keepdims=True)
            done.append(rho * (scaled - unit * mean))
            total = jnp.sum(prod, axis=1, keepdims=True)
            if is_q:
                gain_q = gain_q + total
            else:
                gain_k = gain_k + total
        done.append(d_ref[(heads_q + heads_k) * hd :, :].astype(F32))
        out_ref[0] = jnp.concatenate(done, axis=0).T.astype(BF16)
        lane = lax.broadcasted_iota(jnp.int32, gg_ref.shape, 1)
        gg_ref[...] += jnp.where(lane == 0, gain_q, jnp.where(lane == 1, gain_k, 0.0))

    @pl.when(step == 0)
    def _():
        work(dm_ref, rm_ref)

    @pl.when(step == 1)
    def _():
        work(dt_ref, rt_ref)


def head_back(info, grad_mine, grad_theirs, raw_mine, raw_theirs, cos_part, sin_part, gq, gk, heads):
    cols, tok = grad_mine.shape
    tile = min(512, tok)
    mine = pl.BlockSpec((cols, tile), lambda s, i, info: (0, jnp.where(s == 0, i, tok // tile - 1)))
    theirs = pl.BlockSpec((cols, tile), lambda s, i, info: (0, jnp.where(s == 0, 0, i)))
    tab = lambda a: pl.BlockSpec((a.shape[0], tile), lambda s, i, info: (0, i))
    const = lambda a: pl.BlockSpec(a.shape, lambda s, i, info: (0, 0))
    return pl.pallas_call(
        functools.partial(head_back_kernel, heads),
        grid_spec=pltpu.PrefetchScalarGridSpec(
            num_scalar_prefetch=1,
            grid=(2, tok // tile),
            in_specs=[
                mine,
                theirs,
                mine,
                theirs,
                tab(cos_part),
                tab(sin_part),
                const(gq),
                const(gk),
            ],
            out_specs=[
                pl.BlockSpec(
                    (1, tile, cols), lambda s, i, info: (jnp.bitwise_xor(info[2], s), i, 0)
                ),
                pl.BlockSpec((gq.shape[0], 128), lambda s, i, info: (0, 0)),
            ],
        ),
        out_shape=[shape_of((2, tok, cols), BF16), shape_of((gq.shape[0], 128), F32)],
        compiler_params=settings(2, 60),
        cost_estimate=cost(False),
        name="head_back",
    )(info, grad_mine, grad_theirs, raw_mine, raw_theirs, cos_part, sin_part, gq, gk)


def load_rows(info, mine_ref, got_ref, rows, sems):
    tok = mine_ref.shape[1]
    ctx = info[2]
    here = pl.multiple_of(ctx * tok, tok)
    there = pl.multiple_of((1 - ctx) * tok, tok)
    one = pltpu.make_async_copy(mine_ref, rows.at[:, pl.ds(here, tok)], sems.at[0])
    two = pltpu.make_async_copy(got_ref, rows.at[:, pl.ds(there, tok)], sems.at[1])
    one.start()
    two.start()
    one.wait()
    two.wait()


def keys_with_bias(keys, length):
    hd, slots = keys.shape
    pos = lax.broadcasted_iota(jnp.int32, (hd, slots), 1)
    row = lax.broadcasted_iota(jnp.int32, (hd, slots), 0)
    bias = jnp.where((row == 0) & (pos >= length), NEGATIVE, 0.0)
    return jnp.concatenate([keys.astype(F32), bias], axis=0).T.astype(BF16)


def query_with_one(pair):
    one_row = jnp.where(lax.broadcasted_iota(jnp.int32, pair.shape, 0) == 0, 1.0, 0.0)
    return jnp.concatenate([pair, one_row.astype(BF16)], axis=0)


def causal(scores, width):
    key_pos = lax.broadcasted_iota(jnp.int32, (width, width), 0)
    query_pos = lax.broadcasted_iota(jnp.int32, (width, width), 1)
    allowed = key_pos <= query_pos
    return jnp.where(jnp.concatenate([allowed, allowed], axis=1), scores, NEGATIVE)


def attn_fwd_kernel(
    width, hd, info, mine_ref, got_ref, keep_ref, send_ref, lse_ref, rows, key_rows, sems
):
    head, block = pl.program_id(0), pl.program_id(1)
    heads_k = pl.num_programs(0)
    scale = hd**-0.5 * LOG2E
    length = info[3]
    key_at = pl.multiple_of(heads_k * 2 * hd + head * hd, hd)
    value_at = pl.multiple_of(heads_k * 3 * hd + head * hd, hd)
    query_at = pl.multiple_of(head * 2 * hd, 2 * hd)

    @pl.when((head == 0) & (block == 0))
    def _():
        load_rows(info, mine_ref, got_ref, rows, sems)

    @pl.when(block == 0)
    def _():
        key_rows[...] = keys_with_bias(rows[pl.ds(key_at, hd), :], length)

    start = pl.multiple_of(block * width, width)
    both = rows[pl.ds(query_at, 2 * hd), pl.ds(start, width)]
    query = query_with_one(jnp.concatenate([both[:hd], both[hd:]], axis=1))

    def tile(at, carried, diagonal):
        out, total = carried
        scores = dot(key_rows[pl.ds(at, width), :], query, 1, 0)
        if diagonal:
            scores = causal(scores, width)
        probs = jnp.exp2(scores * scale)
        total = total + jnp.sum(probs, axis=0, keepdims=True)
        out = out + dot(rows[pl.ds(value_at, hd), pl.ds(at, width)], probs.astype(BF16), 1, 0)
        return out, total

    carried = (jnp.zeros((hd, 2 * width), F32), jnp.zeros((1, 2 * width), F32))
    full = jnp.minimum(block, lax.div(length + width - 1, width))
    carried = lax.fori_loop(
        0, full, lambda j, c: tile(pl.multiple_of(j * width, width), c, False), carried
    )
    out, total = tile(start, carried, True)
    out = out * (1.0 / total)
    out = jnp.concatenate([out[:, :width], out[:, width:]], axis=0).T.astype(BF16)
    here = block // 2 == info[2]

    @pl.when(here)
    def _():
        keep_ref[...] = out

    @pl.when(jnp.logical_not(here))
    def _():
        send_ref[...] = out

    log_total = jnp.log2(total)
    lse_ref[0, 0:1, :] = log_total[:, :width]
    lse_ref[0, 1:2, :] = log_total[:, width:]


def keep_block(i, info):
    return jnp.clip(i - 2 * info[2], 0, 1)


def send_block(i, info):
    return jnp.clip(i - 2 * (1 - info[2]), 0, 1)


def attn_fwd(info, mine, got, hd):
    cols, tok = mine.shape
    heads_k = cols // (4 * hd)
    width = tok // 2
    return pl.pallas_call(
        functools.partial(attn_fwd_kernel, width, hd),
        grid_spec=pltpu.PrefetchScalarGridSpec(
            num_scalar_prefetch=1,
            grid=(heads_k, 4),
            in_specs=[ANY, ANY],
            out_specs=[
                pl.BlockSpec((width, 2 * hd), lambda h, i, info: (keep_block(i, info), h)),
                pl.BlockSpec((width, 2 * hd), lambda h, i, info: (send_block(i, info), h)),
                pl.BlockSpec((1, 2, width), lambda h, i, info: (h, 0, i)),
            ],
            scratch_shapes=[
                pltpu.VMEM((cols, 2 * tok), BF16),
                pltpu.VMEM((2 * tok, 2 * hd), BF16),
                pltpu.SemaphoreType.DMA((2,)),
            ],
        ),
        out_shape=[
            shape_of((tok, heads_k * 2 * hd), BF16),
            shape_of((tok, heads_k * 2 * hd), BF16),
            shape_of((heads_k, 2, 2 * tok), F32),
        ],
        compiler_params=settings(2, 60),
        cost_estimate=cost(True),
        name="attn_fwd",
    )(info, mine, got)


def attn_bwd_kernel(
    width,
    hd,
    info,
    mine_ref,
    got_ref,
    ok_ref,
    os_ref,
    gk_ref,
    gs_ref,
    lse_ref,
    keep_ref,
    send_ref,
    rows,
    key_rows,
    value_rows,
    key_sum,
    value_sum,
    sems,
):
    head, block = pl.program_id(0), pl.program_id(1)
    heads_k = pl.num_programs(0)
    scale = hd**-0.5
    length = info[3]
    ctx = info[2]
    tok = keep_ref.shape[1]
    key_at = pl.multiple_of(heads_k * 2 * hd + head * hd, hd)
    value_at = pl.multiple_of(heads_k * 3 * hd + head * hd, hd)
    query_at = pl.multiple_of(head * 2 * hd, 2 * hd)

    @pl.when((head == 0) & (block == 0))
    def _():
        load_rows(info, mine_ref, got_ref, rows, sems)

    @pl.when(block == 0)
    def _():
        key_rows[...] = keys_with_bias(rows[pl.ds(key_at, hd), :], length)
        value_rows[...] = rows[pl.ds(value_at, hd), :].astype(F32).T.astype(BF16)
        key_sum[...] = jnp.zeros_like(key_sum)
        value_sum[...] = jnp.zeros_like(value_sum)

    start = pl.multiple_of(block * width, width)
    here = block // 2 == ctx

    def store_query(value):
        at = pl.ds(pl.multiple_of((block % 2) * width, width), width)

        @pl.when(here)
        def _():
            keep_ref[pl.ds(query_at, 2 * hd), at] = value

        @pl.when(jnp.logical_not(here))
        def _():
            send_ref[pl.ds(query_at, 2 * hd), at] = value

    @pl.when(block * width < length)
    def _():
        both = rows[pl.ds(query_at, 2 * hd), pl.ds(start, width)]
        pair = jnp.concatenate([both[:hd], both[hd:]], axis=1)
        query = query_with_one(pair)
        query_rows = pair.astype(F32).T.astype(BF16)
        grad_wide = jnp.where(here, gk_ref[...].astype(F32), gs_ref[...].astype(F32))
        out_wide = jnp.where(here, ok_ref[...].astype(F32), os_ref[...].astype(F32))
        grad_rows = jnp.concatenate([grad_wide[:, :hd], grad_wide[:, hd:]], axis=0).astype(BF16)
        grad_t = grad_wide.T
        prod = (grad_wide * out_wide).T
        grad = jnp.concatenate([grad_t[:hd], grad_t[hd:]], axis=1).astype(BF16)
        delta = jnp.concatenate(
            [
                jnp.sum(prod[:hd], axis=0, keepdims=True),
                jnp.sum(prod[hd:], axis=0, keepdims=True),
            ],
            axis=1,
        )
        lse = jnp.concatenate([lse_ref[0, 0:1, :], lse_ref[0, 1:2, :]], axis=1)

        def tile(at, query_sum, diagonal):
            scores = dot(key_rows[pl.ds(at, width), :], query, 1, 0)
            if diagonal:
                scores = causal(scores, width)
            probs = jnp.exp2(scores * (scale * LOG2E) - lse)
            grad_probs = dot(value_rows[pl.ds(at, width), :], grad, 1, 0)
            grad_scores = (probs * (grad_probs - delta)).astype(BF16)
            value_sum[pl.ds(at, width), :] += dot(probs.astype(BF16), grad_rows, 1, 0)
            key_sum[pl.ds(at, width), :] += dot(grad_scores, query_rows, 1, 0)
            return query_sum + dot(rows[pl.ds(key_at, hd), pl.ds(at, width)], grad_scores, 1, 0)

        query_sum = lax.fori_loop(
            0,
            block,
            lambda j, s: tile(pl.multiple_of(j * width, width), s, False),
            jnp.zeros((hd, 2 * width), F32),
        )
        query_sum = tile(start, query_sum, True) * scale
        store_query(
            jnp.concatenate([query_sum[:, :width], query_sum[:, width:]], axis=0).astype(BF16)
        )

    @pl.when(block * width >= length)
    def _():
        store_query(jnp.zeros((2 * hd, width), BF16))

    @pl.when(block == 3)
    def _():
        for at, total in ((key_at, key_sum[...] * scale), (value_at, value_sum[...])):
            total = total.T.astype(BF16)
            left, right = total[:, :tok], total[:, tok:]

            @pl.when(ctx == 0)
            def _():
                keep_ref[pl.ds(at, hd), :] = left
                send_ref[pl.ds(at, hd), :] = right

            @pl.when(ctx == 1)
            def _():
                keep_ref[pl.ds(at, hd), :] = right
                send_ref[pl.ds(at, hd), :] = left


def attn_bwd(info, mine, got, out_keep, out_send, grad_keep, grad_send, lse, hd):
    cols, tok = mine.shape
    heads_k = cols // (4 * hd)
    width = tok // 2
    keep = pl.BlockSpec((width, 2 * hd), lambda h, i, info: (keep_block(i, info), h))
    send = pl.BlockSpec((width, 2 * hd), lambda h, i, info: (send_block(i, info), h))
    full = pl.BlockSpec((cols, tok), lambda h, i, info: (0, 0))
    return pl.pallas_call(
        functools.partial(attn_bwd_kernel, width, hd),
        grid_spec=pltpu.PrefetchScalarGridSpec(
            num_scalar_prefetch=1,
            grid=(heads_k, 4),
            in_specs=[
                ANY,
                ANY,
                keep,
                send,
                keep,
                send,
                pl.BlockSpec((1, 2, width), lambda h, i, info: (h, 0, i)),
            ],
            out_specs=[full, full],
            scratch_shapes=[
                pltpu.VMEM((cols, 2 * tok), BF16),
                pltpu.VMEM((2 * tok, 2 * hd), BF16),
                pltpu.VMEM((2 * tok, hd), BF16),
                pltpu.VMEM((2 * tok, hd), F32),
                pltpu.VMEM((2 * tok, hd), F32),
                pltpu.SemaphoreType.DMA((2,)),
            ],
        ),
        out_shape=[shape_of((cols, tok), BF16), shape_of((cols, tok), BF16)],
        compiler_params=settings(2, 60),
        cost_estimate=cost(True),
        name="attn_bwd",
    )(info, mine, got, out_keep, out_send, grad_keep, grad_send, lse)


def load_blocks(plan, pieces, target, sem):
    rows = target.shape[1] // 4

    @pl.when(pl.program_id(0) == 0)
    def _():
        for k, places in enumerate(plan):
            for p, (piece, row) in enumerate(places):
                src = pieces[piece].at[pl.ds(row, rows)]
                pltpu.make_async_copy(src, target.at[k, pl.ds(p * rows, rows)], sem).start()
        pltpu.make_async_copy(target, target, sem).wait()


def out_proj_kernel(plan, count, info, *refs):
    x_ref, a0, a1, b0, b1, gain_ref, r_ref, n_ref, nt_ref, att_ref, w_ref, sem = refs[count:]
    load_blocks(plan, refs, w_ref, sem)
    ctx = info[2]
    total = x_ref[...].astype(F32)
    for j, ref, side in ((0, a0, ctx), (1, a1, ctx), (0, b0, 1 - ctx), (1, b1, 1 - ctx)):
        block = 2 * side + j
        part = ref[...]
        att_ref[block] = part
        total = total + dot(part, w_ref[block], 1, 1)
    rho = lax.rsqrt(jnp.mean(total * total, axis=-1, keepdims=True) + EPS)
    normed = total * rho * gain_ref[...]
    r_ref[...] = total
    n_ref[...] = normed.astype(BF16)
    nt_ref[...] = normed.T.astype(BF16)


def out_proj(info, x, mine, theirs, weights, gain, tile):
    plan, pieces = weights
    tok, width = x.shape
    feats = pieces[0].shape[1]
    rows_of = lambda n: pl.BlockSpec((tile, n), lambda i, info: (i, 0))
    return pl.pallas_call(
        functools.partial(out_proj_kernel, plan, len(pieces)),
        grid_spec=pltpu.PrefetchScalarGridSpec(
            num_scalar_prefetch=1,
            grid=(tok // tile,),
            in_specs=[ANY] * len(pieces)
            + [rows_of(width)]
            + [rows_of(feats)] * 4
            + [pl.BlockSpec((1, width), lambda i, info: (0, 0))],
            out_specs=[
                rows_of(width),
                rows_of(width),
                pl.BlockSpec((width, tile), lambda i, info: (0, i)),
                pl.BlockSpec((4, tile, feats), lambda i, info: (0, i, 0)),
            ],
            scratch_shapes=[pltpu.VMEM((4, width, feats), BF16), pltpu.SemaphoreType.DMA],
        ),
        out_shape=[
            shape_of((tok, width), F32),
            shape_of((tok, width), BF16),
            shape_of((width, tok), BF16),
            shape_of((4, tok, feats), BF16),
        ],
        compiler_params=settings(1, 60),
        cost_estimate=cost(True),
        name="out_proj",
    )(info, *pieces, x, *mine, *theirs, gain)


def norm_two_back_kernel(plan, count, info, *refs):
    g_ref, r_ref, gr_ref, gain_ref, gres_ref, gat_ref, a0, a1, b0, b1, gg_ref, w_ref, sem = refs[count:]
    load_blocks(plan, refs, w_ref, sem)
    ctx = info[2]
    grad, resid = g_ref[...], r_ref[...]
    rho = lax.rsqrt(jnp.mean(resid * resid, axis=-1, keepdims=True) + EPS)
    unit = resid * rho
    scaled = grad * gain_ref[...]
    back = rho * (scaled - unit * jnp.mean(scaled * unit, axis=-1, keepdims=True))
    total = gr_ref[...] + back
    gres_ref[...] = total
    low = total.astype(BF16)
    gat_ref[...] = total.T.astype(BF16)

    @pl.when(pl.program_id(0) == 0)
    def _():
        gg_ref[...] = jnp.zeros_like(gg_ref)

    gg_ref[...] += jnp.sum(grad * unit, axis=0, keepdims=True)
    for j, ref, side in ((0, a0, ctx), (1, a1, ctx), (0, b0, 1 - ctx), (1, b1, 1 - ctx)):
        ref[...] = dot(low, w_ref[2 * side + j], 1, 0).astype(BF16)


def norm_two_back(info, grad, resid, grad_result, gain, weights, tile):
    plan, pieces = weights
    tok, width = grad.shape
    feats = pieces[0].shape[1]
    rows_of = lambda n: pl.BlockSpec((tile, n), lambda i, info: (i, 0))
    row = pl.BlockSpec((1, width), lambda i, info: (0, 0))
    return pl.pallas_call(
        functools.partial(norm_two_back_kernel, plan, len(pieces)),
        grid_spec=pltpu.PrefetchScalarGridSpec(
            num_scalar_prefetch=1,
            grid=(tok // tile,),
            in_specs=[ANY] * len(pieces) + [rows_of(width)] * 3 + [row],
            out_specs=[rows_of(width), pl.BlockSpec((width, tile), lambda i, info: (0, i))]
            + [rows_of(feats)] * 4
            + [row],
            scratch_shapes=[pltpu.VMEM((4, width, feats), BF16), pltpu.SemaphoreType.DMA],
        ),
        out_shape=[shape_of((tok, width), F32), shape_of((width, tok), BF16)]
        + [shape_of((tok, feats), BF16)] * 4
        + [shape_of((1, width), F32)],
        compiler_params=settings(1, 60),
        cost_estimate=cost(True),
        name="norm_two_back",
    )(info, *pieces, grad, resid, grad_result, gain)


def norm_one_back_kernel(plan, count, info, *refs):
    p0, p1, x_ref, gres_ref, gain_ref, *out_refs, gg_ref, w_ref, sem = refs[count:]
    load_blocks(plan, refs, w_ref, sem)
    quarter = x_ref.shape[1] // 4
    grad = dot(p0[0], w_ref[0], 1, 1)
    grad = grad + dot(p1[0], w_ref[1], 1, 1)
    grad = grad + dot(p0[1], w_ref[2], 1, 1)
    grad = grad + dot(p1[1], w_ref[3], 1, 1)
    x = x_ref[...].astype(F32)
    rho = lax.rsqrt(jnp.mean(x * x, axis=-1, keepdims=True) + EPS)
    unit = x * rho
    scaled = grad * gain_ref[...]
    back = rho * (scaled - unit * jnp.mean(scaled * unit, axis=-1, keepdims=True))
    total = (gres_ref[...] + back).astype(BF16)
    for p, mask in enumerate(MASKS):
        at = pl.multiple_of(jnp.bitwise_xor(info[1], mask) * quarter, quarter)
        part = total[:, p * quarter : (p + 1) * quarter]

        for i, out_ref in enumerate(out_refs):

            @pl.when(pl.program_id(0) == i)
            def _():
                out_ref[:, pl.ds(at, quarter)] = part

    @pl.when(pl.program_id(0) == 0)
    def _():
        gg_ref[...] = jnp.zeros_like(gg_ref)

    gg_ref[...] += jnp.sum(grad * unit, axis=0, keepdims=True)


def norm_one_back(info, pairs, weights, x, grad_resid, gain, tile):
    plan, pieces = weights
    tok, width = x.shape
    cols = pieces[0].shape[1]
    rows_of = lambda n: pl.BlockSpec((tile, n), lambda i, info: (i, 0))
    pair = pl.BlockSpec((2, tile, cols), lambda i, info: (0, i, 0))
    row = pl.BlockSpec((1, width), lambda i, info: (0, 0))
    return pl.pallas_call(
        functools.partial(norm_one_back_kernel, plan, len(pieces)),
        grid_spec=pltpu.PrefetchScalarGridSpec(
            num_scalar_prefetch=1,
            grid=(tok // tile,),
            in_specs=[ANY] * len(pieces) + [pair, pair, rows_of(width), rows_of(width), row],
            out_specs=[pl.BlockSpec((tile, width), lambda i, info: (0, 0))] * 4 + [row],
            scratch_shapes=[pltpu.VMEM((4, width, cols), BF16), pltpu.SemaphoreType.DMA],
        ),
        out_shape=[shape_of((tile, width), BF16)] * 4 + [shape_of((1, width), F32)],
        compiler_params=settings(1, 60),
        cost_estimate=cost(True),
        name="norm_one_back",
    )(info, *pieces, *pairs, x, grad_resid, gain)


def weight_copies(plan, pieces, gate_up, down, gate_up_sem, down_sem):
    third = down.shape[1] // 3
    rows = down.shape[0] // 4
    wide, thin = [], []
    for p, chunks in enumerate(plan):
        block = pl.ds(p * rows, rows)
        for j, (piece, row, at) in enumerate(chunks):
            src = pieces[piece].at[pl.ds(row, rows)]
            wide.append(
                pltpu.make_async_copy(
                    src.at[:, pl.ds(at, 2 * third)],
                    gate_up.at[block, pl.ds(j * 2 * third, 2 * third)],
                    gate_up_sem,
                )
            )
            thin.append(
                pltpu.make_async_copy(
                    src.at[:, pl.ds(at + 2 * third, third)],
                    down.at[block, pl.ds(j * third, third)],
                    down_sem,
                )
            )
    return wide, thin


def split_act(act):
    third = act.shape[1] // 6
    part = lambda j: act[:, j * third : (j + 1) * third]
    return [(part(0), part(1)), (part(2), part(3)), (part(4), part(5))]


def ffn_fwd_kernel(tile, plans, last, info, scale, x_ref, in_ref, *rest):
    if last:
        teach_ref, rest = rest[0], rest[1:]
    pieces = []
    for plan in plans:
        count = 1 + max(place[0] for chunks in plan for place in chunks)
        pieces.append(rest[:count])
        rest = rest[count:]
    act_ref, hid_ref = rest[:2]
    if last:
        outa_ref, outb_ref, gres_ref, low_ref, lowt_ref, sq_ref = rest[2:8]
        gate_up, down, total, sems = rest[8:]
    else:
        sum_ref, gate_up, down, total, sems = rest[2:]
    step, part = pl.program_id(0), pl.program_id(1)
    final = len(plans) - 1
    width = x_ref.shape[1]
    quarter = width // 4
    third = down.shape[2] // 3

    def copies(s):
        return weight_copies(
            plans[s], pieces[s], gate_up.at[s], down.at[s], sems.at[s, 0], sems.at[s, 1]
        )

    @pl.when((step == 0) & (part == 0))
    def _():
        for s in range(len(plans)):
            wide, thin = copies(s)
            for copy in wide + thin:
                copy.start()

    for s in range(len(plans)):

        @pl.when((step == s) & (part == 0))
        def _():
            pltpu.make_async_copy(gate_up.at[s], gate_up.at[s], sems.at[s, 0]).wait()

    rows = pl.ds(pl.multiple_of(part * tile, tile), tile)
    act = dot(x_ref[rows, :], gate_up[step], 1, 0)
    for j, (gate, upper) in enumerate(split_act(act)):
        sig = sigmoid(gate)
        silu = gate * sig
        hid_ref[0, :, j * third : (j + 1) * third] = (silu * upper).astype(BF16)
        at = 2 * j * third
        act_ref[0, :, at : at + third] = (upper * (sig + silu - silu * sig)).astype(BF16)
        act_ref[0, :, at + third : at + 2 * third] = silu.astype(BF16)
    for s in range(len(plans)):

        @pl.when((step == s) & (part == 0))
        def _():
            pltpu.make_async_copy(down.at[s], down.at[s], sems.at[s, 1]).wait()

    grown = dot(hid_ref[0], down[step], 1, 1)

    @pl.when(step == 0)
    def _():
        total[rows, :] = in_ref[...] + grown

    @pl.when(step > 0)
    def _():
        total[rows, :] += grown

    @pl.when(step == final)
    def _():
        result = total[rows, :]
        if not last:
            sum_ref[...] = result
            return
        tok = x_ref.shape[0]
        slot = info[2] * tok + part * tile + lax.broadcasted_iota(jnp.int32, (tile, 1), 0)
        valid = jnp.where(slot < info[3], 1.0, 0.0)
        square = jnp.zeros((tile, quarter), F32)
        for p, mask in enumerate(MASKS):
            at = pl.multiple_of(jnp.bitwise_xor(info[1], mask) * quarter, quarter)
            cols = slice(p * quarter, (p + 1) * quarter)
            value = result[:, cols]
            low = value.astype(BF16)

            @pl.when(part < pl.num_programs(1) // 2)
            def _():
                outa_ref[:, pl.ds(at, quarter)] = low

            @pl.when(part >= pl.num_programs(1) // 2)
            def _():
                outb_ref[:, pl.ds(at, quarter)] = low

            error = valid * (value - teach_ref[0, :, pl.ds(at, quarter)].astype(F32))
            square = square + error * error
            grad = error * scale[0]
            gres_ref[:, cols] = grad
            low_ref[:, cols] = grad.astype(BF16)
            lowt_ref[cols, :] = grad.T.astype(BF16)

        @pl.when(part == 0)
        def _():
            sq_ref[...] = jnp.zeros_like(sq_ref)

        sq_ref[...] += jnp.sum(square, axis=0, keepdims=True)


def ffn_fwd(info, scale, x, total, teacher, weights, units, tile):
    tok, width = x.shape
    pieces = [piece for _, group in weights for piece in group]
    count = len(weights)
    last = teacher is not None
    entry = lambda s, i: jnp.where(s == 0, i, tok // tile - 1)
    leave = lambda s, i: jnp.where(s == count - 1, i, 0)
    tiles = lambda n: pl.BlockSpec((tile, n), lambda s, i, info: (leave(s, i), 0))
    slab = lambda n: pl.BlockSpec((1, tile, n), lambda s, i, info: (s, i, 0))
    in_specs = [
        SMEM,
        whole((tok, width)),
        pl.BlockSpec((tile, width), lambda s, i, info: (entry(s, i), 0)),
    ]
    out_specs = [slab(2 * units), slab(units)]
    out_shape = [shape_of((count, tok, 2 * units), BF16), shape_of((count, tok, units), BF16)]
    if last:
        in_specs.append(
            pl.BlockSpec((1, tile, width), lambda s, i, info: (info[0], leave(s, i), 0))
        )
        half = tok // tile // 2
        out_specs += [
            pl.BlockSpec(
                (tile, width), lambda s, i, info: (jnp.minimum(leave(s, i), half - 1), 0)
            ),
            pl.BlockSpec(
                (tile, width), lambda s, i, info: (jnp.maximum(leave(s, i) - half, 0), 0)
            ),
            tiles(width),
            tiles(width),
            pl.BlockSpec((width, tile), lambda s, i, info: (0, leave(s, i))),
            pl.BlockSpec((1, width // 4), lambda s, i, info: (0, 0)),
        ]
        out_shape += [
            shape_of((tok // 2, width), BF16),
            shape_of((tok // 2, width), BF16),
            shape_of((tok, width), F32),
            shape_of((tok, width), BF16),
            shape_of((width, tok), BF16),
            shape_of((1, width // 4), F32),
        ]
    else:
        out_specs.append(tiles(width))
        out_shape.append(shape_of((tok, width), F32))
    return pl.pallas_call(
        functools.partial(ffn_fwd_kernel, tile, [plan for plan, _ in weights], last),
        grid_spec=pltpu.PrefetchScalarGridSpec(
            num_scalar_prefetch=1,
            grid=(count, tok // tile),
            in_specs=in_specs + [ANY] * len(pieces),
            out_specs=out_specs,
            scratch_shapes=[
                pltpu.VMEM((count, width, 2 * units), BF16),
                pltpu.VMEM((count, width, units), BF16),
                pltpu.VMEM((tok, width), F32),
                pltpu.SemaphoreType.DMA((count, 2)),
            ],
        ),
        out_shape=out_shape,
        compiler_params=settings(2, 60),
        cost_estimate=cost(True),
        name="ffn_fwd",
    )(info, scale, x, total, *([teacher] if last else []), *pieces)


def ffn_bwd_kernel(steps, plan, first, low_ref, act_ref, hid_ref, xt_ref, lowt_ref, *rest):
    count = 1 + max(place[0] for chunks in plan for place in chunks)
    pieces, rest = rest[:count], rest[count:]
    if not first:
        in_ref, rest = rest[0], rest[1:]
    out_ref, keep_ref, send_ref, gate_up, down, dact_all, hid_all, sems = rest
    step = pl.program_id(0)
    units = down.shape[1]
    third = units // 3
    tile = low_ref.shape[0]

    @pl.when(step == 0)
    def _():
        wide, thin = weight_copies(plan, pieces, gate_up, down, sems.at[0], sems.at[1])
        for copy in thin + wide:
            copy.start()
        pltpu.make_async_copy(down, down, sems.at[1]).wait()

    @pl.when(step < steps)
    def _():
        rows = pl.ds(pl.multiple_of(step * tile, tile), tile)
        grad_hidden = dot(low_ref[...], down[...], 1, 0)
        for j, (to_gate, to_upper) in enumerate(split_act(act_ref[0])):
            grad = grad_hidden[:, j * third : (j + 1) * third]
            at = 2 * j * third
            dact_all[rows, at : at + third] = (grad * to_gate.astype(F32)).astype(BF16)
            dact_all[rows, at + third : at + 2 * third] = (grad * to_upper.astype(F32)).astype(BF16)
        hid_all[rows, :] = hid_ref[0]

        @pl.when(step == 0)
        def _():
            pltpu.make_async_copy(gate_up, gate_up, sems.at[0]).wait()

        grown = dot(dact_all[rows, :], gate_up[...], 1, 1)
        out_ref[...] = grown if first else in_ref[...] + grown

    def weight_rows(target):
        target[:, : 2 * units] = dot(xt_ref[...], dact_all[...], 1, 0).astype(BF16)
        target[:, 2 * units :] = dot(lowt_ref[...], hid_all[...], 1, 0).astype(BF16)

    @pl.when((step >= steps) & (step < steps + 2))
    def _():
        weight_rows(send_ref)

    @pl.when(step >= steps + 2)
    def _():
        weight_rows(keep_ref)


def ffn_bwd(low, saved, weights, total, xt, lowt, tile):
    plan, pieces = weights
    acts, hiddens, block = saved
    tok, width = low.shape
    units = hiddens.shape[2]
    steps = tok // tile
    quarter = width // 4
    first = total is None
    clip = lambda i: jnp.minimum(i, steps - 1)
    rows_of = lambda n: pl.BlockSpec((tile, n), lambda i: (clip(i), 0))
    slab = lambda n: pl.BlockSpec((1, tile, n), lambda i: (block, clip(i), 0))
    feature = lambda i: (jnp.where(i < steps + 2, jnp.maximum(i - steps, 0) + 2, i - steps - 2), 0)
    return pl.pallas_call(
        functools.partial(ffn_bwd_kernel, steps, plan, first),
        grid=(steps + 4,),
        in_specs=[
            rows_of(width),
            slab(2 * units),
            slab(units),
            pl.BlockSpec((quarter, tok), feature),
            pl.BlockSpec((quarter, tok), feature),
        ]
        + [ANY] * len(pieces)
        + ([] if first else [rows_of(width)]),
        out_specs=[
            rows_of(width),
            pl.BlockSpec((quarter, 3 * units), lambda i: (jnp.maximum(i - steps - 2, 0), 0)),
            pl.BlockSpec((quarter, 3 * units), lambda i: (jnp.clip(i - steps, 0, 1), 0)),
        ],
        out_shape=[
            shape_of((tok, width), F32),
            shape_of((width // 2, 3 * units), BF16),
            shape_of((width // 2, 3 * units), BF16),
        ],
        scratch_shapes=[
            pltpu.VMEM((width, 2 * units), BF16),
            pltpu.VMEM((width, units), BF16),
            pltpu.VMEM((tok, 2 * units), BF16),
            pltpu.VMEM((tok, units), BF16),
            pltpu.SemaphoreType.DMA((2,)),
        ],
        input_output_aliases={} if first else {5 + len(pieces): 0},
        compiler_params=settings(1, 60),
        cost_estimate=cost(True),
        name="ffn_bwd",
    )(low, acts, hiddens, xt, lowt, *pieces, *([] if first else [total]))


def turn_chunks(block):
    wide = block.shape[1] * 2 // 9
    thin = wide // 2
    starts = [(2 * wide, wide), (wide, wide), (0, wide)]
    starts += [(3 * wide + 2 * thin, thin), (3 * wide + thin, thin), (3 * wide, thin)]
    return jnp.concatenate([block[:, a : a + n] for a, n in starts], axis=1)


def sum_kernel(turns, *refs):
    total = None
    for ref, turn in zip(refs[:-1], turns):
        value = ref[...].astype(F32)
        value = turn_chunks(value) if turn else value
        total = value if total is None else total + value
    refs[-1][...] = total.astype(refs[-1].dtype)


def summed(terms, turns=None, dtype=BF16):
    rows, cols = terms[0].shape
    spec = pl.BlockSpec((128, cols), lambda i: (i, 0))
    return pl.pallas_call(
        functools.partial(sum_kernel, turns or [False] * len(terms)),
        grid=(rows // 128,),
        in_specs=[spec] * len(terms),
        out_specs=spec,
        out_shape=shape_of((rows, cols), dtype),
        compiler_params=settings(1, 60),
        cost_estimate=cost(False),
        name="summed",
    )(*terms)


def sums_kernel(jobs, count, info, *refs):
    arrays, refs = refs[:count], refs[count:]
    outs, (term_buf, out_buf, term_sems, out_sems) = refs[: len(jobs)], refs[len(jobs) :]
    rows = term_buf.shape[1]
    copies = []
    for terms in jobs:
        group = []
        for array, base, pick, _ in terms:
            at = base
            if pick is not None:
                at = pl.multiple_of(base + jnp.bitwise_xor(info[2], pick) * rows, rows)
            i = len(copies) + len(group)
            src = arrays[array].at[pl.ds(at, rows)]
            group.append(pltpu.make_async_copy(src, term_buf.at[i], term_sems.at[i]))
            group[-1].start()
        copies += group
    first = 0
    stores = []
    for j, terms in enumerate(jobs):
        total = None
        for i, (_, _, _, turn) in enumerate(terms):
            copies[first + i].wait()
            value = term_buf[first + i].astype(F32)
            value = turn_chunks(value) if turn else value
            total = value if total is None else total + value
        first += len(terms)
        out_buf[j] = total.astype(BF16)
        stores.append(pltpu.make_async_copy(out_buf.at[j], outs[j], out_sems.at[j]))
        stores[-1].start()
    for store in stores:
        store.wait()


def sums(info, arrays, jobs):
    cols = arrays[0].shape[1]
    rows, terms = 128, sum(len(job) for job in jobs)
    return pl.pallas_call(
        functools.partial(sums_kernel, jobs, len(arrays)),
        grid_spec=pltpu.PrefetchScalarGridSpec(
            num_scalar_prefetch=1,
            grid=(1,),
            in_specs=[ANY] * len(arrays),
            out_specs=[ANY] * len(jobs),
            scratch_shapes=[
                pltpu.VMEM((terms, rows, cols), BF16),
                pltpu.VMEM((len(jobs), rows, cols), BF16),
                pltpu.SemaphoreType.DMA((terms,)),
                pltpu.SemaphoreType.DMA((len(jobs),)),
            ],
        ),
        out_shape=[shape_of((rows, cols), BF16)] * len(jobs),
        compiler_params=settings(1, 60),
        cost_estimate=cost(False),
        name="sums",
    )(info, *arrays)


def core_jobs(keep, came):
    return [[(a, far * 256, pick, False) for a in (keep, came)] for far in (0, 1) for pick in (0, 1)]


def core_sum_kernel(info, left_ref, right_ref, *outs):
    total = (left_ref[...].astype(F32) + right_ref[...].astype(F32)).astype(BF16)
    block = pl.program_id(1)
    place = block // 2 * 2 + jnp.bitwise_xor(block % 2, info[2])
    for i, out in enumerate(outs):

        @pl.when(place == i)
        def _():
            out[...] = total


def core_sum(info, keep, came):
    groups, rows, cols = keep.shape
    spec = pl.BlockSpec((1, rows // 4, cols), lambda g, i, info: (g, i, 0))
    return pl.pallas_call(
        core_sum_kernel,
        grid_spec=pltpu.PrefetchScalarGridSpec(
            num_scalar_prefetch=1,
            grid=(groups, 4),
            in_specs=[spec] * 2,
            out_specs=[pl.BlockSpec((1, rows // 4, cols), lambda g, i, info: (g, 0, 0))] * 4,
        ),
        out_shape=[shape_of((groups, rows // 4, cols), BF16)] * 4,
        compiler_params=settings(2, 24),
        cost_estimate=cost(False),
        name="core_sum",
    )(info, keep, came)


def weight_grad_kernel(nt_ref, back0_ref, back1_ref, gt_ref, att_ref, keep_ref, send_ref):
    cols = back0_ref.shape[2]
    part, block = pl.program_id(0), pl.program_id(1)

    def rows(target, back_ref):
        target[0, :, :cols] = dot(nt_ref[...], back_ref[0], 1, 0).astype(BF16)
        target[0, :, cols:] = dot(gt_ref[...], att_ref[0], 1, 0).astype(BF16)

    for j, back_ref in enumerate((back0_ref, back1_ref)):

        @pl.when((part == 0) & (block % 2 == j))
        def _():
            rows(send_ref, back_ref)

        @pl.when((part == 1) & (block % 2 == j))
        def _():
            rows(keep_ref, back_ref)


def weight_grad(normed_t, backs, grad_t, attended):
    width, tok = normed_t.shape
    cols, feats = backs[0].shape[2], attended.shape[2]
    half = pl.BlockSpec((width // 2, tok), lambda p, k: (1 - p, 0))
    side = pl.BlockSpec((1, tok, cols), lambda p, k: (k // 2, 0, 0))
    shape = (1, width // 2, cols + feats)
    return pl.pallas_call(
        weight_grad_kernel,
        grid=(2, 4),
        in_specs=[half, side, side, half, pl.BlockSpec((1, tok, feats), lambda p, k: (k, 0, 0))],
        out_specs=[
            pl.BlockSpec(shape, lambda p, k: (jnp.where(p == 0, 0, k), 0, 0)),
            pl.BlockSpec(shape, lambda p, k: (jnp.where(p == 0, k, 3), 0, 0)),
        ],
        out_shape=[shape_of((4, width // 2, cols + feats), BF16)] * 2,
        compiler_params=settings(2, 60),
        cost_estimate=cost(True),
        name="weight_grad",
    )(normed_t, *backs, grad_t, attended)


def after(value, *others):
    return lax.optimization_barrier((value,) + others)[0]


def per_device_rows(
    tokens,
    teacher,
    lengths,
    attn_gain,
    q_weight,
    k_weight,
    v_weight,
    q_gain,
    k_gain,
    o_weight,
    ffn_gain,
    gate_weight,
    up_weight,
    down_weight,
):
    z = lax.axis_index("tp")
    ctx = lax.axis_index("ctx")
    fsdp = lax.axis_index("fsdp")
    rows_dev, tok, width = tokens.shape
    quarter = width // 4
    hd = q_gain.shape[0] * 4
    q_cols, k_cols = q_weight.shape[1], k_weight.shape[1]
    proj = q_cols + 2 * k_cols
    heads = (q_cols // hd, k_cols // hd)
    units = gate_weight.shape[1]
    slots = rows_dev * 4 * tok * 2

    def x_swap(v):
        return lax.ppermute(v, "fsdp", X_SWAP)

    def core_swap(v):
        return lax.ppermute(v, "fsdp", CORE_SWAP)

    def y_swap(v):
        return lax.ppermute(v, "ctx", Y_SWAP)

    def z_up(v):
        return lax.ppermute(v, "tp", Z_UP)

    def z_far(v):
        return lax.ppermute(v, "tp", Z_FAR)

    def z_down(v):
        return lax.ppermute(v, "tp", Z_DOWN)

    def natural(v):
        v = jnp.concatenate([v[0:1], v[2:3], v[1:2], v[3:4]], axis=0)
        v = jnp.where(fsdp % 2 == 0, v, jnp.concatenate([v[1:2], v[0:1], v[3:4], v[2:3]], axis=0))
        return jnp.where(fsdp // 2 == 0, v, jnp.concatenate([v[2:4], v[0:2]], axis=0))

    v = {}

    def sync():
        v.update(lax.optimization_barrier(dict(v)))

    length = lax.dynamic_slice_in_dim(lengths, z, 1, 0)
    info = jnp.concatenate([jnp.stack([z, fsdp, ctx]).astype(jnp.int32), length])
    w_proj = join(q_weight, k_weight, v_weight)
    proj_z = [z_up(w_proj), z_far(w_proj), z_down(w_proj)]
    proj_far = x_swap(w_proj)
    count_here = jnp.sum(lengths).astype(F32)[None]
    vector = jnp.concatenate([attn_gain, ffn_gain, q_gain, k_gain]).astype(F32)
    vector = jnp.concatenate([vector, count_here, jnp.zeros((640 - 545,), F32)])[None]
    vector = jnp.concatenate([vector, x_swap(vector)], axis=0)
    vector = jnp.concatenate([vector, core_swap(vector)], axis=0)
    w_out, w_ffn, *w_chunks = pack(info, o_weight, gate_weight, up_weight, down_weight)
    pos = (ctx * tok + jnp.arange(tok, dtype=jnp.int32)).astype(F32)
    frequency = THETA ** (-(2.0 * jnp.arange(hd // 2, dtype=F32)) / hd)
    angles = frequency[:, None] * pos[None, :]
    head_gains = natural(vector[:, 2 * quarter : 544])
    v.update(
        info=info,
        proj_own=jnp.concatenate([w_proj, proj_far], axis=0),
        proj_z=jnp.concatenate(proj_z, axis=0),
        w_out=w_out,
        w_ffn=w_ffn,
        w_chunks=w_chunks,
        gain_one=vector[:, :quarter].reshape(1, width),
        gain_two=vector[:, quarter : 2 * quarter].reshape(1, width),
        total_count=jnp.sum(vector[:, 544]),
        gain_q=head_gains[:, : hd // 4].reshape(hd, 1),
        gain_k=head_gains[:, hd // 4 :].reshape(hd, 1),
        cos_part=jnp.cos(angles),
        sin_part=jnp.sin(angles),
    )
    sync()
    info = v["info"]

    proj_zfar = x_swap(v["proj_z"])
    out_z = [z_up(v["w_out"]), z_far(v["w_out"]), z_down(v["w_out"])]
    own_core = core_swap(v["proj_own"])
    x_in, normed_one_t = norm_one(info, tokens, v["gain_one"], 256)
    v.update(
        proj_zfar=proj_zfar,
        own_core=own_core,
        x_in=x_in,
        normed_one_t=normed_one_t,
        out_z=out_z,
    )
    sync()

    plan_proj = [[(0, 0), (0, quarter), (3, 0), (3, quarter)]]
    plan_proj += [[(p, k * quarter) for p in (1, 2, 4, 5)] for k in range(3)]
    weights_proj = [v["proj_own"], v["proj_z"], v["proj_zfar"], v["own_core"]]
    weights_proj += [core_swap(v["proj_z"]), core_swap(v["proj_zfar"])]
    one = [z_up(v["w_chunks"][0]), z_up(v["w_chunks"][3])]
    ffn_far = x_swap(v["w_ffn"])
    tables = [v[name] for name in ("cos_part", "sin_part", "gain_q", "gain_k")]

    def make(block, *then):
        normed_t = after(v["normed_one_t"], *then)
        return project(info, (plan_proj, weights_proj), normed_t, *tables, heads, block)

    theirs = [make(lambda s: 2 * (1 - s[2]))]
    got = [y_swap(theirs[0][0])]
    theirs.append(make(lambda s: 2 * (1 - s[2]) + 1, theirs[0][0]))
    got.append(y_swap(theirs[1][0]))
    mine = [make(lambda s: 2 * s[2], theirs[1][0])]
    mine.append(make(lambda s: 2 * s[2] + 1, mine[0][0]))
    v.update(
        one=one,
        ffn_far=ffn_far,
        weights_proj=weights_proj,
        mine=mine,
        theirs=theirs,
        got0=got[0],
    )
    sync()

    one_far = [x_swap(v["one"][0])]
    three = [z_down(v["w_chunks"][0])]
    own_cores = [core_swap(v["w_ffn"]), core_swap(v["ffn_far"])]
    first = attn_fwd(info, v["mine"][0][0], v["got0"], hd)
    v.update(first=first, got1=got[1], one_far=one_far, three=three, own_cores=own_cores)
    sync()

    arrived = [y_swap(v["first"][1])]
    three = v["three"] + [z_down(v["w_chunks"][1])]
    out_blocks = jnp.concatenate([v["w_out"]] + v["out_z"], axis=0)
    out_far = x_swap(out_blocks)
    one_cores = [core_swap(v["one"][0]), core_swap(v["one_far"][0])]
    second = attn_fwd(info, v["mine"][1][0], v["got1"], hd)
    v.update(
        second=second,
        arrived=arrived,
        three=three,
        out_blocks=out_blocks,
        out_far=out_far,
        one_cores=one_cores,
    )
    sync()

    arrived = v["arrived"] + [y_swap(v["second"][1])]
    three = v["three"] + [z_down(v["w_chunks"][2])]
    one_far = v["one_far"] + [x_swap(v["one"][1][:, :units])]
    weights_out = [v["out_blocks"], v["out_far"]]
    weights_out += [core_swap(v["out_blocks"]), core_swap(v["out_far"])]
    v.update(arrived=arrived, three=three, one_far=one_far, weights_out=weights_out)
    sync()

    plan_out = [[(p, k * quarter) for p in range(4)] for k in range(4)]
    two = [z_up(v["one"][0])]
    three_far = [x_swap(v["three"][0])]
    one_far = v["one_far"] + [y_swap(v["one_far"][0])]
    one_cores = v["one_cores"] + [core_swap(v["one"][1]), core_swap(v["one_far"][1])]
    resid, normed_two, normed_two_t, attended = out_proj(
        info,
        v["x_in"],
        [v["first"][0], v["second"][0]],
        v["arrived"],
        (plan_out, v["weights_out"]),
        v["gain_two"],
        256,
    )
    v.update(
        two=two,
        three_far=three_far,
        one_far=one_far,
        one_cores=one_cores,
        resid=resid,
        normed_two=normed_two,
        normed_two_t=normed_two_t,
        attended=attended,
    )
    sync()

    plan0 = [[(i, 0, j * units) for j in range(3)] for i in range(4)]
    plan_mixed = [[(0, 0, 0), (1, 0, 0), (1, 0, units)], [(i, 0, 0) for i in (2, 3, 4)]]
    plan_mixed += [[(5, 0, 0), (6, 0, 0), (6, 0, units)], [(i, 0, 0) for i in (7, 8, 9)]]
    scale = (slots / v["total_count"])[None]
    weights0 = [v["w_ffn"], v["ffn_far"]] + v["own_cores"]
    c0, cf, c1, cb = v["one_cores"]
    weights1 = v["one"] + v["one_far"] + [c0, c1, cf, cb, core_swap(v["one_far"][2])]
    two = v["two"] + [z_up(v["one"][1])]
    three_far = v["three_far"] + [x_swap(v["three"][1]), y_swap(v["three_far"][0])]
    two_far = [x_swap(v["two"][0])]
    three_cores = [core_swap(v["three"][0])]
    acts_a, hiddens_a, sum_a = ffn_fwd(
        info,
        scale,
        v["normed_two"],
        v["resid"],
        None,
        [(plan0, weights0), (plan_mixed, weights1)],
        units,
        256,
    )
    v.update(
        scale=scale,
        weights0=weights0,
        weights1=weights1,
        two=two,
        three_far=three_far,
        two_far=two_far,
        three_cores=three_cores,
        acts_a=acts_a,
        hiddens_a=hiddens_a,
        sum_a=sum_a,
    )
    sync()

    plan_chunks = [[(3 * p + j, 0, 0) for j in range(3)] for p in range(4)]
    weights3 = v["three"] + v["three_far"] + v["three_cores"]
    weights3 += [core_swap(part) for part in v["three"][1:]]
    weights3 += [core_swap(part) for part in v["three_far"]]
    two_far = v["two_far"] + [x_swap(v["two"][1][:, :units]), y_swap(v["two_far"][0])]
    two_cores = [core_swap(part) for part in v["two"] + v["two_far"]]
    acts_b, hiddens_b, sum_b = ffn_fwd(
        info, v["scale"], v["normed_two"], v["sum_a"], None, [(plan_chunks, weights3)], units, 256
    )
    v.update(
        weights3=weights3,
        two_far=two_far,
        two_cores=two_cores,
        acts_b=acts_b,
        hiddens_b=hiddens_b,
        sum_b=sum_b,
    )
    sync()

    weights2 = v["two"] + v["two_far"] + v["two_cores"]
    weights2 += [core_swap(part) for part in v["two_far"][1:]]
    acts_c, hiddens_c, *results, grad_result, grad_low, grad_low_t, square = ffn_fwd(
        info, v["scale"], v["normed_two"], v["sum_b"], teacher, [(plan_mixed, weights2)], units, 256
    )
    v.update(
        weights2=weights2,
        acts_c=acts_c,
        hiddens_c=hiddens_c,
        results=results,
        grad_result=grad_result,
        grad_low=grad_low,
        grad_low_t=grad_low_t,
        square=square,
    )
    sync()

    def ffn_back(plan, weights, acts, hiddens, block, total):
        return ffn_bwd(
            v["grad_low"],
            (v[acts], v[hiddens], block),
            (plan, v[weights]),
            total,
            v["normed_two_t"],
            v["grad_low_t"],
            256,
        )

    turned = [False, False, True]
    one = [z_up(v["results"][0])]
    total, keep2, send2 = ffn_back(plan_mixed, "weights2", "acts_c", "hiddens_c", 0, None)
    v.update(one=one, total=total, keep2=keep2, send2=send2)
    sync()

    one = v["one"] + [z_up(v["results"][1])]
    came2 = core_swap(v["send2"])
    total, keep1, send1 = ffn_back(plan_mixed, "weights1", "acts_a", "hiddens_a", 1, v["total"])
    v.update(one=one, came2=came2, total=total, keep1=keep1, send1=send1)
    sync()

    out_three = [z_down(v["results"][0])]
    came1 = core_swap(v["send1"])
    sum2 = sums(info, [v["keep2"], v["came2"]], core_jobs(0, 1))
    far_t2 = x_swap(sum2[3])
    total, keep3, send3 = ffn_back(
        plan_chunks, "weights3", "acts_b", "hiddens_b", 0, after(v["total"], sum2[0])
    )
    v.update(
        out_three=out_three,
        came1=came1,
        sum2=sum2,
        far_t2=far_t2,
        total=total,
        keep3=keep3,
        send3=send3,
    )
    sync()

    out_three = v["out_three"] + [z_down(v["results"][1])]
    came3 = core_swap(v["send3"])
    far_h2 = x_swap(v["sum2"][2])
    there2, *sum1 = sums(
        info,
        [v["sum2"][1], v["far_t2"], v["keep1"], v["came1"]],
        [[(0, 0, None, False), (1, 0, None, False)]] + core_jobs(2, 3),
    )
    there2 = y_swap(there2)
    total, keep0, send0 = ffn_back(
        plan0, "weights0", "acts_a", "hiddens_a", 0, after(v["total"], sum1[0])
    )
    v.update(
        out_three=out_three,
        came3=came3,
        far_h2=far_h2,
        there2=there2,
        sum1=sum1,
        total=total,
        keep0=keep0,
        send0=send0,
    )
    sync()

    came0 = core_swap(v["send0"])
    far_t1 = x_swap(v["sum1"][3])
    plane = [(0, 0, None, False), (1, 0, None, False), (2, 0, None, True)]
    part2, *sum3 = sums(
        info,
        [v["sum2"][0], v["far_h2"], v["there2"], v["keep3"], v["came3"]],
        [plane] + core_jobs(3, 4),
    )
    down2 = z_down(part2)
    grad_resid, grad_attn_t, a0, a1, b0, b1, gain_two_sum = norm_two_back(
        info,
        after(v["total"], sum3[0]),
        v["resid"],
        v["grad_result"],
        v["gain_two"],
        (plan_out, v["weights_out"]),
        256,
    )
    grad_got = [y_swap(b0), y_swap(b1)]
    v.update(
        came0=came0,
        far_t1=far_t1,
        down2=down2,
        sum3=sum3,
        grad_resid=grad_resid,
        grad_attn_t=grad_attn_t,
        grad_mine=[a0, a1],
        gain_two_sum=gain_two_sum,
        grad_got0=grad_got[0],
    )
    sync()

    def attn_back(j, grad):
        out, got_ref = v["first" if j == 0 else "second"], v[f"got{j}"]
        return attn_bwd(
            info, v["mine"][j][0], got_ref, out[0], out[1], grad, v[f"grad_got{j}"], out[2], hd
        )

    two = [z_up(v["one"][0])]
    far_h1 = x_swap(v["sum1"][2])
    there1, *sum0 = sums(
        info,
        [v["sum1"][1], v["far_t1"], v["keep0"], v["came0"]],
        [[(0, 0, None, False), (1, 0, None, False)]] + core_jobs(2, 3),
    )
    there1 = y_swap(there1)
    far_t3 = x_swap(v["sum3"][3])
    back0 = attn_back(0, after(v["grad_mine"][0], sum0[0]))
    v.update(
        out_two=two,
        far_h1=far_h1,
        there1=there1,
        far_t3=far_t3,
        sum0=sum0,
        back0=back0,
        grad_got1=grad_got[1],
    )
    sync()

    two = v["out_two"] + [z_up(v["one"][1])]
    heads0 = y_swap(v["back0"][1])
    far_h3 = x_swap(v["sum3"][2])
    far_t0 = x_swap(v["sum0"][3])
    there3, two_down = sums(
        info,
        [v["sum3"][1], v["far_t3"], v["sum1"][0], v["far_h1"], v["there1"], v["down2"]],
        [
            [(0, 0, None, False), (1, 0, None, False)],
            [(2, 0, None, False), (3, 0, None, False), (4, 0, None, True), (5, 0, None, False)],
        ],
    )
    there3_got = y_swap(there3)
    two_down_got = z_down(two_down)
    back1 = attn_back(1, after(v["grad_mine"][1], there3, two_down))
    v.update(
        out_two=two, heads0=heads0, far_h3=far_h3, far_t0=far_t0, there3=there3_got, back1=back1
    )
    sync()

    heads1 = y_swap(v["back1"][1])
    far_h0 = x_swap(v["sum0"][2])
    part3, there0 = sums(
        info,
        [v["sum3"][0], v["far_h3"], v["there3"], v["sum0"][1], v["far_t0"]],
        [plane, [(3, 0, None, False), (4, 0, None, False)]],
    )
    up3 = z_up(part3)
    tables = [v[name] for name in ("cos_part", "sin_part", "gain_q", "gain_k")]
    head0 = head_back(
        info, v["back0"][0], v["heads0"], v["mine"][0][1], v["theirs"][0][1], *tables, heads
    )
    v.update(heads1=heads1, two_down=two_down_got, head0=head0, there0=there0)
    sync()

    there0 = y_swap(v["there0"])
    head1 = head_back(
        info, v["back1"][0], v["heads1"], v["mine"][1][1], v["theirs"][1][1], *tables, heads
    )
    *tokens_low, gain_one_sum = norm_one_back(
        info,
        [v["head0"][0], head1[0]],
        (plan_proj, v["weights_proj"]),
        v["x_in"],
        v["grad_resid"],
        v["gain_one"],
        tok // 4,
    )
    v.update(head1=head1, tokens_low=tokens_low, gain_one_sum=gain_one_sum, up3=up3)
    v.update(there0=there0, far_h0=far_h0)
    sync()

    def place(out, parts, k, first):
        row = lax.rem(z - k + 4, 4)
        for j, part in enumerate(parts):
            at = (first + j) * part.shape[0]
            out = lax.dynamic_update_slice(out, part.astype(out.dtype)[None], (row, at, 0))
        return out

    v.update(out_one=v["one"])
    quarters = v["tokens_low"]
    one = [z_up(quarters[0])]
    keep, send = weight_grad(
        v["normed_one_t"], [v["head0"][0], v["head1"][0]], v["grad_attn_t"], v["attended"]
    )
    gain_heads = v["head0"][1] + v["head1"][1]
    vector = jnp.concatenate(
        [
            natural(v["gain_one_sum"].reshape(4, quarter)).reshape(1, width),
            natural(v["gain_two_sum"].reshape(4, quarter)).reshape(1, width),
            gain_heads[:, 0].reshape(1, hd),
            gain_heads[:, 1].reshape(1, hd),
            jnp.sum(v["square"]).reshape(1, 1),
            jnp.zeros((1, 127), F32),
        ],
        axis=1,
    )
    vector = vector + core_swap(vector)
    v.update(one=one, keep=keep, send=send)
    v.update(vector=vector)
    sync()

    one = v["one"] + [z_up(v["tokens_low"][1])]
    rows = quarter // 2
    flat = lambda a: a.reshape(4 * rows, a.shape[-1])
    attn_sums = [flat(p) for p in core_sum(info, v["keep"], core_swap(v["send"]))]
    vector = v["vector"] + x_swap(v["vector"])
    v.update(one=one, sums=attn_sums, vector=vector)
    sync()

    one = v["one"] + [z_up(v["tokens_low"][2])]
    far_t = x_swap(v["sums"][3])
    part0 = summed([v["sum0"][0], v["far_h0"], v["there0"]], turned)
    ffn_sum = summed([part0, v["two_down"], v["up3"]], None, F32)
    vector = v["vector"] + y_swap(v["vector"])
    v.update(one=one, far_t=far_t, ffn_sum=ffn_sum, vector=vector)
    sync()

    one = v["one"] + [z_up(v["tokens_low"][3])]
    three = [z_down(v["tokens_low"][0])]
    far_h = x_swap(v["sums"][2])
    there = y_swap(summed([v["sums"][1], v["far_t"]]))
    output = jnp.zeros((rows_dev, tok, width), BF16)
    for k, parts in enumerate((v["results"], v["out_one"], v["out_two"], v["out_three"])):
        output = place(output, parts, k, 0)
    v.update(one=one, three=three, far_h=far_h, there=there, output=output)
    sync()

    three = v["three"] + [z_down(v["tokens_low"][1])]
    parts = summed([v["sums"][0], v["far_h"], v["there"]])
    parts = [parts[k * rows : (k + 1) * rows] for k in range(4)]
    parts = [parts[0], z_down(parts[1]), z_far(parts[2]), z_up(parts[3])]
    ffn_other = y_swap(v["ffn_sum"])
    grad = place(jnp.zeros((rows_dev, tok, width), F32), v["tokens_low"], 0, 0)
    v.update(three=three, parts=parts, grad=grad)
    sync()

    three = v["three"] + [z_down(part) for part in v["tokens_low"][2:]]
    attn_sum = summed(v["parts"], None, F32)
    vector = v["vector"] + lax.ppermute(v["vector"], "tp", Z_NEAR)
    grad = place(v["grad"], v["one"], 1, 0)
    v.update(three=three, attn_sum=attn_sum, vector=vector, grad=grad, ffn_other=ffn_other)
    sync()

    def finish(own, other):
        return jnp.concatenate(
            [jnp.where(ctx == 0, own, other), jnp.where(ctx == 0, other, own)], axis=0
        )

    def columns(first):
        parts = [ffn_grad[:, first(j) : first(j) + third] for j in range(3)]
        return jnp.concatenate(
            [
                jnp.where(ctx == 0, parts[0], parts[2]),
                parts[1],
                jnp.where(ctx == 0, parts[2], parts[0]),
            ],
            axis=1,
        )

    two = [z_up(part) for part in v["one"][:2]]
    third = units // 3
    ffn_grad = finish(v["ffn_sum"], turn_chunks(v["ffn_other"]))
    grad_gate = columns(lambda j: 2 * j * third)
    grad_up = columns(lambda j: (2 * j + 1) * third)
    grad_down = columns(lambda j: 2 * units + j * third).T
    attn_other = y_swap(v["attn_sum"])
    vector = v["vector"] + lax.ppermute(v["vector"], "tp", Z_FAR)
    grad = place(v["grad"], v["three"], 3, 0)
    v.update(two=two, vector=vector, grad=grad, attn_other=attn_other)
    v.update(grad_gate=grad_gate, grad_up=grad_up, grad_down=grad_down)
    sync()

    two = [z_up(part) for part in v["one"][2:]]
    tokens_grad = place(place(v["grad"], v["two"], 2, 0), two, 2, 2)
    output = v["output"]
    sums_all = v["vector"][0]

    attn_grad = finish(v["attn_sum"], v["attn_other"])
    teacher_loss = sums_all[2 * width + 2 * hd] / (v["total_count"] * width)

    def own_part(at, size):
        return lax.dynamic_slice_in_dim(sums_all, at + fsdp * (size // 4), size // 4, 0)

    return (
        output,
        teacher_loss,
        tokens_grad,
        own_part(0, width),
        attn_grad[:, :q_cols],
        attn_grad[:, q_cols : q_cols + k_cols],
        attn_grad[:, q_cols + k_cols : proj],
        own_part(2 * width, hd),
        own_part(2 * width + hd, hd),
        attn_grad[:, proj:].T,
        own_part(width, width),
        v["grad_gate"],
        v["grad_up"],
        v["grad_down"],
    )


def solution(mesh):
    return jax.shard_map(
        per_device_rows if fits(mesh) else per_device_any,
        mesh=mesh,
        in_specs=(
            P("fsdp", "ctx", None),
            P("fsdp", "ctx", None),
            P("fsdp"),
            P("fsdp"),
            P("fsdp", "tp"),
            P("fsdp", "tp"),
            P("fsdp", "tp"),
            P("fsdp"),
            P("fsdp"),
            P("tp", "fsdp"),
            P("fsdp"),
            P("fsdp", "tp"),
            P("fsdp", "tp"),
            P("tp", "fsdp"),
        ),
        out_specs=(
            P("fsdp", "ctx", None),
            P(),
            P("fsdp", "ctx", None),
            P("fsdp"),
            P("fsdp", "tp"),
            P("fsdp", "tp"),
            P("fsdp", "tp"),
            P("fsdp"),
            P("fsdp"),
            P("tp", "fsdp"),
            P("fsdp"),
            P("fsdp", "tp"),
            P("fsdp", "tp"),
            P("tp", "fsdp"),
        ),
        check_vma=False,
    )
```

```python
import functools
import math

import jax
import jax.numpy as jnp
from jax import lax
from jax.experimental import pallas as pl
from jax.experimental.pallas import tpu as pltpu
from jax.sharding import PartitionSpec as P

EPS = 1e-05
THETA = 1000000.0
NEGATIVE = -1e30


def rms_scale(field_in, gain_vec):
    return (
        field_in * lax.rsqrt(jnp.mean(field_in * field_in, axis=-1, keepdims=True) + EPS) * gain_vec
    )


def rotate(field_in, positions):
    half_dim = field_in.shape[-1] // 2
    frequency = THETA ** (-(2.0 * jnp.arange(half_dim, dtype=jnp.float32)) / field_in.shape[-1])
    angles = positions[:, None] * frequency[None, :]
    cos_part = jnp.cos(angles)[:, None, :]
    sin_part = jnp.sin(angles)[:, None, :]
    lower_half = field_in[..., :half_dim]
    upper_half = field_in[..., half_dim:]
    return jnp.concatenate(
        [
            lower_half * cos_part - upper_half * sin_part,
            upper_half * cos_part + lower_half * sin_part,
        ],
        axis=-1,
    )


def linear(left_mat, right_mat):
    return jnp.dot(left_mat, right_mat, preferred_element_type=jnp.float32)


def linear_left(left_mat, right_mat):
    return lax.dot_general(
        left_mat, right_mat, (((0,), (0,)), ((), ())), preferred_element_type=jnp.float32
    )


def linear_right(left_mat, right_mat):
    return lax.dot_general(
        left_mat, right_mat, (((1,), (1,)), ((), ())), preferred_element_type=jnp.float32
    )


def swiglu(gate_act, up_act):
    return jax.nn.silu(gate_act) * up_act


def per_device_any(
    tokens,
    teacher,
    lengths,
    attn_gain,
    q_weight,
    k_weight,
    v_weight,
    q_gain,
    k_gain,
    o_weight,
    ffn_gain,
    gate_weight,
    up_weight,
    down_weight,
):
    (
        gain_one,
        w_query,
        w_key,
        w_value,
        gain_query,
        gain_key,
        w_output,
        gain_two,
        w_gate,
        w_upper,
        w_down,
    ) = (
        lax.all_gather(attn_gain, "fsdp", axis=0, tiled=True),
        lax.all_gather(q_weight, "fsdp", axis=0, tiled=True),
        lax.all_gather(k_weight, "fsdp", axis=0, tiled=True),
        lax.all_gather(v_weight, "fsdp", axis=0, tiled=True),
        lax.all_gather(q_gain, "fsdp", axis=0, tiled=True),
        lax.all_gather(k_gain, "fsdp", axis=0, tiled=True),
        lax.all_gather(o_weight, "fsdp", axis=1, tiled=True),
        lax.all_gather(ffn_gain, "fsdp", axis=0, tiled=True),
        lax.all_gather(gate_weight, "fsdp", axis=0, tiled=True),
        lax.all_gather(up_weight, "fsdp", axis=0, tiled=True),
        lax.all_gather(down_weight, "fsdp", axis=1, tiled=True),
    )
    rows_dev, block_len, model_width = tokens.shape
    count_tok = rows_dev * block_len
    head_dim = gain_query.shape[0]
    q_heads = w_query.shape[1] // head_dim
    kv_heads = w_key.shape[1] // head_dim
    group_size = q_heads // kv_heads
    score_scale = head_dim ** (-0.5)
    row_len = block_len * lax.axis_size("ctx")
    key_block = math.gcd(row_len, 512)
    block_start = lax.axis_index("ctx") * block_len
    tiles_used = (block_start + block_len + key_block - 1) // key_block
    slot_pos = block_start + jnp.arange(block_len, dtype=jnp.int32)
    positions = slot_pos.astype(jnp.float32)
    valid = (slot_pos[None, :] < lengths[:, None]).astype(jnp.float32)
    slots = count_tok * lax.axis_size("fsdp") * lax.axis_size("ctx")
    gain_two_f = gain_two.astype(jnp.float32)
    gain_one_f = gain_one.astype(jnp.float32)
    inputs = tokens.astype(jnp.float32)
    normed_one, back_one = jax.vjp(rms_scale, inputs, gain_one_f)
    normed_low = normed_one.astype(jnp.bfloat16).reshape(count_tok, model_width)
    query_raw = linear(normed_low, w_query)
    key_raw = linear(normed_low, w_key)
    value_raw = linear(normed_low, w_value)

    def heads_post(raw_heads, gain_vec):
        shaped = raw_heads.reshape(rows_dev, block_len, -1, head_dim)
        return rotate(rms_scale(shaped, gain_vec), positions)

    query_rot, query_back = jax.vjp(heads_post, query_raw, gain_query.astype(jnp.float32))
    key_rot, key_back = jax.vjp(heads_post, key_raw, gain_key.astype(jnp.float32))
    queries = query_rot.astype(jnp.bfloat16).reshape(
        rows_dev, block_len, kv_heads, group_size, head_dim
    )
    key_rows = key_rot.astype(jnp.bfloat16).reshape(rows_dev, block_len, kv_heads * head_dim)
    values = value_raw.astype(jnp.bfloat16).reshape(rows_dev, block_len, kv_heads * head_dim)
    keys_all, values_all = (
        lax.all_gather(key_rows, "ctx", axis=1, tiled=True),
        lax.all_gather(values, "ctx", axis=1, tiled=True),
    )

    def key_tile(tile_index):
        tile_start = tile_index * key_block
        key_pos = tile_start + jnp.arange(key_block, dtype=jnp.int32)
        key_part = lax.dynamic_slice_in_dim(keys_all, tile_start, key_block, 1).reshape(
            rows_dev, key_block, kv_heads, head_dim
        )
        value_part = lax.dynamic_slice_in_dim(values_all, tile_start, key_block, 1).reshape(
            rows_dev, key_block, kv_heads, head_dim
        )
        scores = (
            jnp.einsum("rqhgd,rkhd->rhgqk", queries, key_part, preferred_element_type=jnp.float32)
            * score_scale
        )
        allowed = (key_pos[None, None, :] <= slot_pos[None, :, None]) & (
            key_pos[None, None, :] < lengths[:, None, None]
        )
        return (tile_start, scores, allowed[:, None, None], key_part, value_part)

    stat_shape = (rows_dev, kv_heads, group_size, block_len)

    def stats_step(tile_index, carried):
        running_max, running_sum = carried
        tile_start, scores, allowed, key_part, value_part = key_tile(tile_index)
        masked = jnp.where(allowed, scores, NEGATIVE)
        new_max = jnp.maximum(running_max, jnp.max(masked, axis=-1))
        terms = jnp.where(allowed, jnp.exp(masked - new_max[..., None]), 0.0)
        return (new_max, running_sum * jnp.exp(running_max - new_max) + jnp.sum(terms, axis=-1))

    running_max, running_sum = lax.fori_loop(
        0,
        tiles_used,
        stats_step,
        (jnp.full(stat_shape, NEGATIVE, jnp.float32), jnp.zeros(stat_shape, jnp.float32)),
    )
    log_total = running_max + jnp.log(running_sum)
    out_shape = (rows_dev, block_len, kv_heads, group_size, head_dim)

    def value_step(tile_index, carried):
        rounded_out, exact_out = carried
        tile_start, scores, allowed, key_part, value_part = key_tile(tile_index)
        tile_probs = jnp.where(allowed, jnp.exp(scores - log_total[..., None]), 0.0)
        rounded_out = rounded_out + jnp.einsum(
            "rhgqk,rkhd->rqhgd",
            tile_probs.astype(jnp.bfloat16),
            value_part,
            preferred_element_type=jnp.float32,
        )
        exact_out = exact_out + jnp.einsum(
            "rhgqk,rkhd->rqhgd", tile_probs, value_part.astype(jnp.float32)
        )
        return (rounded_out, exact_out)

    rounded_out, exact_out = lax.fori_loop(
        0,
        tiles_used,
        value_step,
        (jnp.zeros(out_shape, jnp.float32), jnp.zeros(out_shape, jnp.float32)),
    )
    attended = rounded_out.astype(jnp.bfloat16).reshape(count_tok, q_heads * head_dim)
    attn_total = lax.psum(linear(attended, w_output), "tp")
    resid = inputs + attn_total.reshape(rows_dev, block_len, model_width)
    normed_two, back_two = jax.vjp(rms_scale, resid, gain_two_f)
    normed_second = normed_two.astype(jnp.bfloat16).reshape(count_tok, model_width)
    gate_act = linear(normed_second, w_gate)
    up_act = linear(normed_second, w_upper)
    hidden_full, back_glu = jax.vjp(swiglu, gate_act, up_act)
    hidden = hidden_full.astype(jnp.bfloat16)
    ffn_total = lax.psum(linear(hidden, w_down), "tp")
    result = resid + ffn_total.reshape(rows_dev, block_len, model_width)
    error_value = result - teacher.astype(jnp.float32)
    valid_col = valid[..., None]
    total_square, total_count = lax.psum(
        (jnp.sum(valid_col * error_value * error_value), jnp.sum(valid)), ("fsdp", "ctx")
    )
    teacher_loss = total_square / (total_count * model_width)
    grad_result = valid_col * error_value * (slots / total_count)
    grad_low = grad_result.astype(jnp.bfloat16).reshape(count_tok, model_width)
    grad_down = linear_left(hidden, grad_low)
    grad_hidden = linear_right(grad_low, w_down)
    grad_gate_full, grad_up_full = back_glu(grad_hidden)
    grad_gate = grad_gate_full.astype(jnp.bfloat16)
    grad_up = grad_up_full.astype(jnp.bfloat16)
    grad_wgate = linear_left(normed_second, grad_gate)
    grad_wup = linear_left(normed_second, grad_up)
    normed_two_part = linear_right(grad_gate, w_gate) + linear_right(grad_up, w_upper)
    grad_normed_two = lax.psum(normed_two_part, "tp")
    grad_resid_norm, grad_gain_two = back_two(
        grad_normed_two.reshape(rows_dev, block_len, model_width)
    )
    grad_resid = grad_result + grad_resid_norm
    grad_attn_low = grad_resid.astype(jnp.bfloat16).reshape(count_tok, model_width)
    grad_woutput = linear_left(attended, grad_attn_low)
    grad_attended = linear_right(grad_attn_low, w_output).astype(jnp.bfloat16).reshape(out_shape)
    delta = jnp.einsum("rqhgd,rqhgd->rhgq", grad_attended.astype(jnp.float32), exact_out)
    full_shape = (rows_dev, row_len, kv_heads * head_dim)

    def grad_step(tile_index, carried):
        grad_queries, grad_keys, grad_values = carried
        tile_start, scores, allowed, key_part, value_part = key_tile(tile_index)
        tile_probs = jnp.where(allowed, jnp.exp(scores - log_total[..., None]), 0.0)
        grad_probs = jnp.einsum(
            "rqhgd,rkhd->rhgqk", grad_attended, value_part, preferred_element_type=jnp.float32
        )
        grad_scores = (tile_probs * (grad_probs - delta[..., None])).astype(jnp.bfloat16)
        grad_queries = (
            grad_queries
            + jnp.einsum(
                "rhgqk,rkhd->rqhgd", grad_scores, key_part, preferred_element_type=jnp.float32
            )
            * score_scale
        )
        key_term = (
            jnp.einsum(
                "rhgqk,rqhgd->rkhd", grad_scores, queries, preferred_element_type=jnp.float32
            )
            * score_scale
        )
        value_term = jnp.einsum(
            "rhgqk,rqhgd->rkhd",
            tile_probs.astype(jnp.bfloat16),
            grad_attended,
            preferred_element_type=jnp.float32,
        )
        grad_keys = lax.dynamic_update_slice_in_dim(
            grad_keys, key_term.reshape(rows_dev, key_block, kv_heads * head_dim), tile_start, 1
        )
        grad_values = lax.dynamic_update_slice_in_dim(
            grad_values, value_term.reshape(rows_dev, key_block, kv_heads * head_dim), tile_start, 1
        )
        return (grad_queries, grad_keys, grad_values)

    grad_queries, grad_keys, grad_values = lax.fori_loop(
        0,
        tiles_used,
        grad_step,
        (
            jnp.zeros(out_shape, jnp.float32),
            jnp.zeros(full_shape, jnp.float32),
            jnp.zeros(full_shape, jnp.float32),
        ),
    )
    key_grad, value_grad = (
        lax.psum_scatter(grad_keys, "ctx", scatter_dimension=1, tiled=True),
        lax.psum_scatter(grad_values, "ctx", scatter_dimension=1, tiled=True),
    )
    grad_query_raw, grad_gain_query = query_back(
        grad_queries.reshape(rows_dev, block_len, q_heads, head_dim)
    )
    grad_key_raw, grad_gain_key = key_back(
        key_grad.reshape(rows_dev, block_len, kv_heads, head_dim)
    )
    query_low = grad_query_raw.astype(jnp.bfloat16)
    key_low = grad_key_raw.astype(jnp.bfloat16)
    value_low = value_grad.reshape(count_tok, kv_heads * head_dim).astype(jnp.bfloat16)
    grad_wquery = linear_left(normed_low, query_low)
    grad_wkey = linear_left(normed_low, key_low)
    grad_wvalue = linear_left(normed_low, value_low)
    normed_part = (
        linear_right(query_low, w_query)
        + linear_right(key_low, w_key)
        + linear_right(value_low, w_value)
    )
    grad_normed_one, grad_gain_query, grad_gain_key = lax.psum(
        (normed_part, grad_gain_query, grad_gain_key), "tp"
    )
    grad_input_norm, grad_gain_one = back_one(
        grad_normed_one.reshape(rows_dev, block_len, model_width)
    )
    tokens_grad = grad_resid + grad_input_norm
    partials = (
        grad_gain_one,
        grad_wquery,
        grad_wkey,
        grad_wvalue,
        grad_gain_query,
        grad_gain_key,
        grad_woutput,
        grad_gain_two,
        grad_wgate,
        grad_wup,
        grad_down,
    )
    pieces = (
        lax.psum_scatter(partials[0], ("fsdp", "ctx"), scatter_dimension=0, tiled=True),
        lax.psum_scatter(partials[1], ("fsdp", "ctx"), scatter_dimension=0, tiled=True),
        lax.psum_scatter(partials[2], ("fsdp", "ctx"), scatter_dimension=0, tiled=True),
        lax.psum_scatter(partials[3], ("fsdp", "ctx"), scatter_dimension=0, tiled=True),
        lax.psum_scatter(partials[4], ("fsdp", "ctx"), scatter_dimension=0, tiled=True),
        lax.psum_scatter(partials[5], ("fsdp", "ctx"), scatter_dimension=0, tiled=True),
        lax.psum_scatter(partials[6], ("fsdp", "ctx"), scatter_dimension=1, tiled=True),
        lax.psum_scatter(partials[7], ("fsdp", "ctx"), scatter_dimension=0, tiled=True),
        lax.psum_scatter(partials[8], ("fsdp", "ctx"), scatter_dimension=0, tiled=True),
        lax.psum_scatter(partials[9], ("fsdp", "ctx"), scatter_dimension=0, tiled=True),
        lax.psum_scatter(partials[10], ("fsdp", "ctx"), scatter_dimension=1, tiled=True),
    )
    summed = (
        lax.all_gather(pieces[0], "ctx", axis=0, tiled=True),
        lax.all_gather(pieces[1], "ctx", axis=0, tiled=True),
        lax.all_gather(pieces[2], "ctx", axis=0, tiled=True),
        lax.all_gather(pieces[3], "ctx", axis=0, tiled=True),
        lax.all_gather(pieces[4], "ctx", axis=0, tiled=True),
        lax.all_gather(pieces[5], "ctx", axis=0, tiled=True),
        lax.all_gather(pieces[6], "ctx", axis=1, tiled=True),
        lax.all_gather(pieces[7], "ctx", axis=0, tiled=True),
        lax.all_gather(pieces[8], "ctx", axis=0, tiled=True),
        lax.all_gather(pieces[9], "ctx", axis=0, tiled=True),
        lax.all_gather(pieces[10], "ctx", axis=1, tiled=True),
    )
    return (
        result.astype(jnp.bfloat16),
        teacher_loss,
        tokens_grad,
        summed[0],
        summed[1],
        summed[2],
        summed[3],
        summed[4],
        summed[5],
        summed[6],
        summed[7],
        summed[8],
        summed[9],
        summed[10],
    )


BF16 = jnp.bfloat16
F32 = jnp.float32
LOG2E = math.log2(math.e)
X_SWAP = [(0, 2), (2, 0), (1, 3), (3, 1)]
CORE_SWAP = [(0, 1), (1, 0), (2, 3), (3, 2)]
Y_SWAP = [(0, 1), (1, 0)]
Z_UP = [(0, 1), (1, 2), (2, 3), (3, 0)]
Z_DOWN = [(0, 3), (1, 0), (2, 1), (3, 2)]
Z_NEAR = [(0, 1), (1, 0), (2, 3), (3, 2)]
Z_FAR = [(0, 2), (2, 0), (1, 3), (3, 1)]
MASKS = (0, 2, 1, 3)
ANY = pl.BlockSpec(memory_space=pl.ANY)
SMEM = pl.BlockSpec(memory_space=pltpu.SMEM)


def fits(mesh):
    return dict(mesh.shape) == {"fsdp": 4, "ctx": 2, "tp": 4}


def dot(left, right, left_dim, right_dim):
    return lax.dot_general(
        left, right, (((left_dim,), (right_dim,)), ((), ())), preferred_element_type=F32
    )


def sigmoid(v):
    return 0.5 * jnp.tanh(0.5 * v) + 0.5


def whole(shape):
    zeros = (0,) * len(shape)
    return pl.BlockSpec(shape, lambda *_: zeros, pipeline_mode=pl.Buffered(1))


def settings(dims, mib):
    return pltpu.CompilerParams(
        dimension_semantics=("arbitrary",) * dims, vmem_limit_bytes=mib << 20
    )


def shape_of(shape, dtype):
    return jax.ShapeDtypeStruct(shape, dtype)


def cost(large):
    size = 1 << 42 if large else 1 << 10
    return pl.CostEstimate(flops=size, bytes_accessed=size >> 12, transcendentals=0)


def pack_kernel(info, o_in, g_in, u_in, d_in, *refs):
    out_ref, ffn_ref, *chunk_refs, others_ref, o_ref, g_ref, u_ref, d_ref, sems = refs
    ctx = info[2]
    pairs = ((o_in, o_ref), (g_in, g_ref), (u_in, u_ref), (d_in, d_ref))
    copies = [pltpu.make_async_copy(a, b, sems.at[i]) for i, (a, b) in enumerate(pairs)]
    for copy in copies:
        copy.start()
    for copy in copies:
        copy.wait()
    out_ref[...] = o_ref[...].astype(F32).T.astype(BF16)
    third = g_ref.shape[1] // 3
    for j in range(3):
        at = pl.multiple_of(jnp.where(ctx == 0, j, 2 - j) * third, third)
        parts = [
            g_ref[:, pl.ds(at, third)],
            u_ref[:, pl.ds(at, third)],
            d_ref[pl.ds(at, third), :].astype(F32).T.astype(BF16),
        ]
        for i, part in enumerate(parts):
            chunk_refs[j][:, i * third : (i + 1) * third] = part
            if j:
                others_ref[:, (3 * j - 3 + i) * third : (3 * j - 2 + i) * third] = part
            ffn_ref[:, (3 * j + i) * third : (3 * j + i + 1) * third] = part


def pack(info, o, g, u, d):
    rows, units = g.shape
    feats = o.shape[0]
    widths = (feats, 3 * units, units, units, units, 2 * units)
    return pl.pallas_call(
        pack_kernel,
        in_specs=[SMEM] + [ANY] * 4,
        out_specs=[pl.BlockSpec(memory_space=pltpu.VMEM)] * 6,
        out_shape=[shape_of((rows, n), BF16) for n in widths],
        scratch_shapes=[pltpu.VMEM(a.shape, BF16) for a in (o, g, u, d)]
        + [pltpu.SemaphoreType.DMA((4,))],
        compiler_params=pltpu.CompilerParams(vmem_limit_bytes=24 << 20),
        cost_estimate=cost(False),
        name="pack",
    )(info, o, g, u, d)


def join_kernel(q_ref, k_ref, v_ref, out_ref):
    at = 0
    for ref in (q_ref, k_ref, v_ref):
        out_ref[:, at : at + ref.shape[1]] = ref[...]
        at += ref.shape[1]


def join(q, k, v):
    return pl.pallas_call(
        join_kernel,
        out_shape=shape_of((q.shape[0], q.shape[1] + k.shape[1] + v.shape[1]), BF16),
        compiler_params=pltpu.CompilerParams(vmem_limit_bytes=8 << 20),
        cost_estimate=cost(False),
        name="join",
    )(q, k, v)


def norm_one_kernel(info, tok_ref, gain_ref, x_ref, nt_ref, x32):
    quarter = x_ref.shape[1] // 4
    for p, mask in enumerate(MASKS):
        at = pl.multiple_of(jnp.bitwise_xor(info[1], mask) * quarter, quarter)
        part = tok_ref[0, :, pl.ds(at, quarter)]
        x_ref[:, p * quarter : (p + 1) * quarter] = part
        x32[:, p * quarter : (p + 1) * quarter] = part.astype(F32)
    x = x32[...]
    rho = lax.rsqrt(jnp.mean(x * x, axis=-1, keepdims=True) + EPS)
    nt_ref[...] = (x * rho * gain_ref[...]).T.astype(BF16)


def norm_one(info, tokens, gain, tile):
    _, tok, width = tokens.shape
    return pl.pallas_call(
        norm_one_kernel,
        grid_spec=pltpu.PrefetchScalarGridSpec(
            num_scalar_prefetch=1,
            grid=(tok // tile,),
            in_specs=[
                pl.BlockSpec((1, tile, width), lambda i, info: (info[0], i, 0)),
                pl.BlockSpec((1, width), lambda i, info: (0, 0)),
            ],
            out_specs=[
                pl.BlockSpec((tile, width), lambda i, info: (i, 0)),
                pl.BlockSpec((width, tile), lambda i, info: (0, i)),
            ],
            scratch_shapes=[pltpu.VMEM((tile, width), F32)],
        ),
        out_shape=[shape_of((tok, width), BF16), shape_of((width, tok), BF16)],
        compiler_params=settings(1, 24),
        cost_estimate=cost(False),
        name="norm_one",
    )(info, tokens, gain)


def proj_kernel(heads, block, plan, count, info, *refs):
    nt_ref, cos_ref, sin_ref, qg_ref, kg_ref, rot_ref, raw_ref, w_ref, sem = refs[count:]
    rows = w_ref.shape[0] // 4

    @pl.when(pl.program_id(0) == 0)
    def _():
        for k in range(4):

            @pl.when(block(info) == k)
            def _():
                for p, (piece, row) in enumerate(plan[k]):
                    src = refs[piece].at[pl.ds(row, rows)]
                    pltpu.make_async_copy(src, w_ref.at[pl.ds(p * rows, rows)], sem).start()

        pltpu.make_async_copy(w_ref, w_ref, sem).wait()

    hd = qg_ref.shape[0]
    half = hd // 2
    raw = dot(w_ref[...], nt_ref[...], 0, 0)
    cos_part, sin_part = cos_ref[...], sin_ref[...]
    heads_q, heads_k = heads
    raw_ref[...] = raw.astype(BF16)
    for h in range(heads_q + heads_k):
        v = raw[h * hd : (h + 1) * hd]
        rho = lax.rsqrt(jnp.mean(v * v, axis=0, keepdims=True) + EPS)
        v = v * rho * (qg_ref[...] if h < heads_q else kg_ref[...])
        a, b = v[:half], v[half:]
        rot_ref[h * hd : h * hd + half, :] = (a * cos_part - b * sin_part).astype(BF16)
        rot_ref[h * hd + half : (h + 1) * hd, :] = (b * cos_part + a * sin_part).astype(BF16)
    at = (heads_q + heads_k) * hd
    rot_ref[at:, :] = raw[at:].astype(BF16)


def project(info, weights, normed_t, cos_part, sin_part, gain_q, gain_k, heads, block):
    plan, pieces = weights
    width, tok = normed_t.shape
    cols = pieces[0].shape[1]
    tile = min(512, tok)
    const = lambda a: pl.BlockSpec(a.shape, lambda i, info: (0, 0))
    tab = lambda a: pl.BlockSpec((a.shape[0], tile), lambda i, info: (0, i))
    return pl.pallas_call(
        functools.partial(proj_kernel, heads, block, plan, len(pieces)),
        grid_spec=pltpu.PrefetchScalarGridSpec(
            num_scalar_prefetch=1,
            grid=(tok // tile,),
            in_specs=[ANY] * len(pieces)
            + [tab(normed_t), tab(cos_part), tab(sin_part), const(gain_q), const(gain_k)],
            out_specs=[pl.BlockSpec((cols, tile), lambda i, info: (0, i))] * 2,
            scratch_shapes=[pltpu.VMEM((width, cols), BF16), pltpu.SemaphoreType.DMA],
        ),
        out_shape=[shape_of((cols, tok), BF16), shape_of((cols, tok), BF16)],
        compiler_params=settings(1, 24),
        cost_estimate=cost(False),
        name="project",
    )(info, *pieces, normed_t, cos_part, sin_part, gain_q, gain_k)


def head_back_kernel(
    heads, info, dm_ref, dt_ref, rm_ref, rt_ref, cos_ref, sin_ref, qg_ref, kg_ref, out_ref, gg_ref
):
    step, part = pl.program_id(0), pl.program_id(1)
    hd = qg_ref.shape[0]
    half = hd // 2
    heads_q, heads_k = heads
    cos_part, sin_part = cos_ref[...], sin_ref[...]
    tile = cos_part.shape[1]

    @pl.when((step == 0) & (part == 0))
    def _():
        gg_ref[...] = jnp.zeros_like(gg_ref)

    def work(d_ref, r_ref):
        gain_q = jnp.zeros((hd, 1), F32)
        gain_k = jnp.zeros((hd, 1), F32)
        done = []
        for h in range(heads_q + heads_k):
            is_q = h < heads_q
            g = d_ref[h * hd : (h + 1) * hd, :].astype(F32)
            raw = r_ref[h * hd : (h + 1) * hd, :].astype(F32)
            a, b = g[:half], g[half:]
            turned = jnp.concatenate(
                [a * cos_part + b * sin_part, b * cos_part - a * sin_part], axis=0
            )
            rho = lax.rsqrt(jnp.mean(raw * raw, axis=0, keepdims=True) + EPS)
            unit = raw * rho
            prod = turned * unit
            scaled = turned * (qg_ref[...] if is_q else kg_ref[...])
            mean = jnp.mean(scaled * unit, axis=0, keepdims=True)
            done.append(rho * (scaled - unit * mean))
            total = jnp.sum(prod, axis=1, keepdims=True)
            if is_q:
                gain_q = gain_q + total
            else:
                gain_k = gain_k + total
        done.append(d_ref[(heads_q + heads_k) * hd :, :].astype(F32))
        out_ref[0] = jnp.concatenate(done, axis=0).T.astype(BF16)
        lane = lax.broadcasted_iota(jnp.int32, gg_ref.shape, 1)
        gg_ref[...] += jnp.where(lane == 0, gain_q, jnp.where(lane == 1, gain_k, 0.0))

    @pl.when(step == 0)
    def _():
        work(dm_ref, rm_ref)

    @pl.when(step == 1)
    def _():
        work(dt_ref, rt_ref)


def head_back(info, grad_mine, grad_theirs, raw_mine, raw_theirs, cos_part, sin_part, gq, gk, heads):
    cols, tok = grad_mine.shape
    tile = min(512, tok)
    mine = pl.BlockSpec((cols, tile), lambda s, i, info: (0, jnp.where(s == 0, i, tok // tile - 1)))
    theirs = pl.BlockSpec((cols, tile), lambda s, i, info: (0, jnp.where(s == 0, 0, i)))
    tab = lambda a: pl.BlockSpec((a.shape[0], tile), lambda s, i, info: (0, i))
    const = lambda a: pl.BlockSpec(a.shape, lambda s, i, info: (0, 0))
    return pl.pallas_call(
        functools.partial(head_back_kernel, heads),
        grid_spec=pltpu.PrefetchScalarGridSpec(
            num_scalar_prefetch=1,
            grid=(2, tok // tile),
            in_specs=[
                mine,
                theirs,
                mine,
                theirs,
                tab(cos_part),
                tab(sin_part),
                const(gq),
                const(gk),
            ],
            out_specs=[
                pl.BlockSpec(
                    (1, tile, cols), lambda s, i, info: (jnp.bitwise_xor(info[2], s), i, 0)
                ),
                pl.BlockSpec((gq.shape[0], 128), lambda s, i, info: (0, 0)),
            ],
        ),
        out_shape=[shape_of((2, tok, cols), BF16), shape_of((gq.shape[0], 128), F32)],
        compiler_params=settings(2, 60),
        cost_estimate=cost(False),
        name="head_back",
    )(info, grad_mine, grad_theirs, raw_mine, raw_theirs, cos_part, sin_part, gq, gk)


def load_rows(info, mine_ref, got_ref, rows, sems):
    tok = mine_ref.shape[1]
    ctx = info[2]
    here = pl.multiple_of(ctx * tok, tok)
    there = pl.multiple_of((1 - ctx) * tok, tok)
    one = pltpu.make_async_copy(mine_ref, rows.at[:, pl.ds(here, tok)], sems.at[0])
    two = pltpu.make_async_copy(got_ref, rows.at[:, pl.ds(there, tok)], sems.at[1])
    one.start()
    two.start()
    one.wait()
    two.wait()


def keys_with_bias(keys, length):
    hd, slots = keys.shape
    pos = lax.broadcasted_iota(jnp.int32, (hd, slots), 1)
    row = lax.broadcasted_iota(jnp.int32, (hd, slots), 0)
    bias = jnp.where((row == 0) & (pos >= length), NEGATIVE, 0.0)
    return jnp.concatenate([keys.astype(F32), bias], axis=0).T.astype(BF16)


def query_with_one(pair):
    one_row = jnp.where(lax.broadcasted_iota(jnp.int32, pair.shape, 0) == 0, 1.0, 0.0)
    return jnp.concatenate([pair, one_row.astype(BF16)], axis=0)


def by_halves(left, right):
    half = left.shape[1] // 2
    return jnp.concatenate(
        [left[:, :half], right[:, :half], left[:, half:], right[:, half:]], axis=1
    )


def by_heads(both):
    quarter = both.shape[1] // 4
    part = lambda i: both[:, i * quarter : (i + 1) * quarter]
    return (
        jnp.concatenate([part(0), part(2)], axis=1),
        jnp.concatenate([part(1), part(3)], axis=1),
    )


def causal(scores):
    half = scores.shape[0]
    key_pos = lax.broadcasted_iota(jnp.int32, (half, half), 0)
    query_pos = lax.broadcasted_iota(jnp.int32, (half, half), 1)
    allowed = key_pos <= query_pos
    return jnp.where(jnp.concatenate([allowed, allowed], axis=1), scores, NEGATIVE)


def attn_fwd_kernel(
    width, hd, info, mine_ref, got_ref, keep_ref, send_ref, lse_ref, rows, key_rows, sems
):
    head, block = pl.program_id(0), pl.program_id(1)
    heads_k = pl.num_programs(0)
    scale = hd**-0.5 * LOG2E
    length = info[3]
    key_at = pl.multiple_of(heads_k * 2 * hd + head * hd, hd)
    value_at = pl.multiple_of(heads_k * 3 * hd + head * hd, hd)
    query_at = pl.multiple_of(head * 2 * hd, 2 * hd)

    @pl.when((head == 0) & (block == 0))
    def _():
        load_rows(info, mine_ref, got_ref, rows, sems)

    @pl.when(block == 0)
    def _():
        key_rows[...] = keys_with_bias(rows[pl.ds(key_at, hd), :], length)

    start = pl.multiple_of(block * width, width)
    both = rows[pl.ds(query_at, 2 * hd), pl.ds(start, width)]
    query = query_with_one(by_halves(both[:hd], both[hd:]))
    half = width // 2

    def terms(at, keys, query, mask):
        scores = dot(key_rows[pl.ds(at, keys), :], query, 1, 0)
        if mask:
            part = causal(scores[:, :width])
            wide = scores.shape[1] > width
            scores = jnp.concatenate([part, scores[:, width:]], axis=1) if wide else part
        probs = jnp.exp2(scores * scale)
        total = jnp.sum(probs, axis=0, keepdims=True)
        return dot(rows[pl.ds(value_at, hd), pl.ds(at, keys)], probs.astype(BF16), 1, 0), total

    def tile(at, carried):
        more, sums = terms(at, width, query, False)
        return carried[0] + more, carried[1] + sums

    carried = (jnp.zeros((hd, 2 * width), F32), jnp.zeros((1, 2 * width), F32))
    full = jnp.minimum(block, lax.div(length + width - 1, width))
    carried = lax.fori_loop(
        0, full, lambda j, c: tile(pl.multiple_of(j * width, width), c), carried
    )
    more, sums = terms(start, half, query, True)
    out, total = carried[0] + more, carried[1] + sums
    later = pl.multiple_of(start + half, half)
    more, sums = terms(later, half, query[:, width:], True)
    out = jnp.concatenate([out[:, :width], out[:, width:] + more], axis=1)
    total = jnp.concatenate([total[:, :width], total[:, width:] + sums], axis=1)
    out = out * (1.0 / total)
    out = jnp.concatenate(by_heads(out), axis=0).T.astype(BF16)
    here = block // 2 == info[2]

    @pl.when(here)
    def _():
        keep_ref[...] = out

    @pl.when(jnp.logical_not(here))
    def _():
        send_ref[...] = out

    log_first, log_second = by_heads(jnp.log2(total))
    lse_ref[0, 0:1, :] = log_first
    lse_ref[0, 1:2, :] = log_second


def keep_block(i, info):
    return jnp.clip(i - 2 * info[2], 0, 1)


def send_block(i, info):
    return jnp.clip(i - 2 * (1 - info[2]), 0, 1)


def attn_fwd(info, mine, got, hd):
    cols, tok = mine.shape
    heads_k = cols // (4 * hd)
    width = tok // 2
    return pl.pallas_call(
        functools.partial(attn_fwd_kernel, width, hd),
        grid_spec=pltpu.PrefetchScalarGridSpec(
            num_scalar_prefetch=1,
            grid=(heads_k, 4),
            in_specs=[ANY, ANY],
            out_specs=[
                pl.BlockSpec((width, 2 * hd), lambda h, i, info: (keep_block(i, info), h)),
                pl.BlockSpec((width, 2 * hd), lambda h, i, info: (send_block(i, info), h)),
                pl.BlockSpec((1, 2, width), lambda h, i, info: (h, 0, i)),
            ],
            scratch_shapes=[
                pltpu.VMEM((cols, 2 * tok), BF16),
                pltpu.VMEM((2 * tok, 2 * hd), BF16),
                pltpu.SemaphoreType.DMA((2,)),
            ],
        ),
        out_shape=[
            shape_of((tok, heads_k * 2 * hd), BF16),
            shape_of((tok, heads_k * 2 * hd), BF16),
            shape_of((heads_k, 2, 2 * tok), F32),
        ],
        compiler_params=settings(2, 60),
        cost_estimate=cost(True),
        name="attn_fwd",
    )(info, mine, got)


def attn_bwd_kernel(
    width,
    hd,
    info,
    mine_ref,
    got_ref,
    ok_ref,
    os_ref,
    gk_ref,
    gs_ref,
    lse_ref,
    keep_ref,
    send_ref,
    rows,
    key_rows,
    value_rows,
    key_sum,
    value_sum,
    sems,
):
    head, block = pl.program_id(0), pl.program_id(1)
    heads_k = pl.num_programs(0)
    scale = hd**-0.5
    length = info[3]
    ctx = info[2]
    tok = keep_ref.shape[1]
    key_at = pl.multiple_of(heads_k * 2 * hd + head * hd, hd)
    value_at = pl.multiple_of(heads_k * 3 * hd + head * hd, hd)
    query_at = pl.multiple_of(head * 2 * hd, 2 * hd)

    @pl.when((head == 0) & (block == 0))
    def _():
        load_rows(info, mine_ref, got_ref, rows, sems)

    @pl.when(block == 0)
    def _():
        key_rows[...] = keys_with_bias(rows[pl.ds(key_at, hd), :], length)
        value_rows[...] = rows[pl.ds(value_at, hd), :].astype(F32).T.astype(BF16)
        key_sum[...] = jnp.zeros_like(key_sum)
        value_sum[...] = jnp.zeros_like(value_sum)

    start = pl.multiple_of(block * width, width)
    here = block // 2 == ctx

    def store_query(value):
        at = pl.ds(pl.multiple_of((block % 2) * width, width), width)

        @pl.when(here)
        def _():
            keep_ref[pl.ds(query_at, 2 * hd), at] = value

        @pl.when(jnp.logical_not(here))
        def _():
            send_ref[pl.ds(query_at, 2 * hd), at] = value

    @pl.when(block * width < length)
    def _():
        both = rows[pl.ds(query_at, 2 * hd), pl.ds(start, width)]
        pair = by_halves(both[:hd], both[hd:])
        query = query_with_one(pair)
        query_rows = pair.astype(F32).T.astype(BF16)
        grad_wide = jnp.where(here, gk_ref[...].astype(F32), gs_ref[...].astype(F32))
        out_wide = jnp.where(here, ok_ref[...].astype(F32), os_ref[...].astype(F32))
        grad_t = grad_wide.T
        prod = (grad_wide * out_wide).T
        grad = by_halves(grad_t[:hd], grad_t[hd:]).astype(BF16)
        half = width // 2
        grad_rows = jnp.concatenate(
            [
                grad_wide[:half, :hd],
                grad_wide[:half, hd:],
                grad_wide[half:, :hd],
                grad_wide[half:, hd:],
            ],
            axis=0,
        ).astype(BF16)
        delta = by_halves(
            jnp.sum(prod[:hd], axis=0, keepdims=True), jnp.sum(prod[hd:], axis=0, keepdims=True)
        )
        lse = by_halves(lse_ref[0, 0:1, :], lse_ref[0, 1:2, :])

        def terms(at, keys, first, mask):
            scores = dot(key_rows[pl.ds(at, keys), :], query[:, first:], 1, 0)
            if mask:
                part = causal(scores[:, :width])
                wide = scores.shape[1] > width
                scores = jnp.concatenate([part, scores[:, width:]], axis=1) if wide else part
            probs = jnp.exp2(scores * (scale * LOG2E) - lse[:, first:])
            grad_probs = dot(value_rows[pl.ds(at, keys), :], grad[:, first:], 1, 0)
            grad_scores = (probs * (grad_probs - delta[:, first:])).astype(BF16)
            value_sum[pl.ds(at, keys), :] += dot(probs.astype(BF16), grad_rows[first:], 1, 0)
            key_sum[pl.ds(at, keys), :] += dot(grad_scores, query_rows[first:], 1, 0)
            return dot(rows[pl.ds(key_at, hd), pl.ds(at, keys)], grad_scores, 1, 0)

        query_sum = lax.fori_loop(
            0,
            block,
            lambda j, s: s + terms(pl.multiple_of(j * width, width), width, 0, False),
            jnp.zeros((hd, 2 * width), F32),
        )
        query_sum = query_sum + terms(start, half, 0, True)
        later = terms(pl.multiple_of(start + half, half), half, width, True)
        query_sum = jnp.concatenate([query_sum[:, :width], query_sum[:, width:] + later], axis=1)
        store_query(jnp.concatenate(by_heads(query_sum * scale), axis=0).astype(BF16))

    @pl.when(block * width >= length)
    def _():
        store_query(jnp.zeros((2 * hd, width), BF16))

    @pl.when(block == 3)
    def _():
        for at, total in ((key_at, key_sum[...] * scale), (value_at, value_sum[...])):
            total = total.T.astype(BF16)
            left, right = total[:, :tok], total[:, tok:]

            @pl.when(ctx == 0)
            def _():
                keep_ref[pl.ds(at, hd), :] = left
                send_ref[pl.ds(at, hd), :] = right

            @pl.when(ctx == 1)
            def _():
                keep_ref[pl.ds(at, hd), :] = right
                send_ref[pl.ds(at, hd), :] = left


def attn_bwd(info, mine, got, out_keep, out_send, grad_keep, grad_send, lse, hd):
    cols, tok = mine.shape
    heads_k = cols // (4 * hd)
    width = tok // 2
    keep = pl.BlockSpec((width, 2 * hd), lambda h, i, info: (keep_block(i, info), h))
    send = pl.BlockSpec((width, 2 * hd), lambda h, i, info: (send_block(i, info), h))
    full = pl.BlockSpec((cols, tok), lambda h, i, info: (0, 0))
    return pl.pallas_call(
        functools.partial(attn_bwd_kernel, width, hd),
        grid_spec=pltpu.PrefetchScalarGridSpec(
            num_scalar_prefetch=1,
            grid=(heads_k, 4),
            in_specs=[
                ANY,
                ANY,
                keep,
                send,
                keep,
                send,
                pl.BlockSpec((1, 2, width), lambda h, i, info: (h, 0, i)),
            ],
            out_specs=[full, full],
            scratch_shapes=[
                pltpu.VMEM((cols, 2 * tok), BF16),
                pltpu.VMEM((2 * tok, 2 * hd), BF16),
                pltpu.VMEM((2 * tok, hd), BF16),
                pltpu.VMEM((2 * tok, hd), F32),
                pltpu.VMEM((2 * tok, hd), F32),
                pltpu.SemaphoreType.DMA((2,)),
            ],
        ),
        out_shape=[shape_of((cols, tok), BF16), shape_of((cols, tok), BF16)],
        compiler_params=settings(2, 60),
        cost_estimate=cost(True),
        name="attn_bwd",
    )(info, mine, got, out_keep, out_send, grad_keep, grad_send, lse)


def load_blocks(plan, pieces, target, sem):
    rows = target.shape[1] // 4

    @pl.when(pl.program_id(0) == 0)
    def _():
        for k, places in enumerate(plan):
            for p, (piece, row) in enumerate(places):
                src = pieces[piece].at[pl.ds(row, rows)]
                pltpu.make_async_copy(src, target.at[k, pl.ds(p * rows, rows)], sem).start()
        pltpu.make_async_copy(target, target, sem).wait()


def out_proj_kernel(plan, count, info, *refs):
    x_ref, a0, a1, b0, b1, gain_ref, r_ref, n_ref, nt_ref, att_ref, w_ref, sem = refs[count:]
    load_blocks(plan, refs, w_ref, sem)
    ctx = info[2]
    total = x_ref[...].astype(F32)
    for j, ref, side in ((0, a0, ctx), (1, a1, ctx), (0, b0, 1 - ctx), (1, b1, 1 - ctx)):
        block = 2 * side + j
        part = ref[...]
        att_ref[block] = part
        total = total + dot(part, w_ref[block], 1, 1)
    rho = lax.rsqrt(jnp.mean(total * total, axis=-1, keepdims=True) + EPS)
    normed = total * rho * gain_ref[...]
    r_ref[...] = total
    n_ref[...] = normed.astype(BF16)
    nt_ref[...] = normed.T.astype(BF16)


def out_proj(info, x, mine, theirs, weights, gain, tile):
    plan, pieces = weights
    tok, width = x.shape
    feats = pieces[0].shape[1]
    rows_of = lambda n: pl.BlockSpec((tile, n), lambda i, info: (i, 0))
    return pl.pallas_call(
        functools.partial(out_proj_kernel, plan, len(pieces)),
        grid_spec=pltpu.PrefetchScalarGridSpec(
            num_scalar_prefetch=1,
            grid=(tok // tile,),
            in_specs=[ANY] * len(pieces)
            + [rows_of(width)]
            + [rows_of(feats)] * 4
            + [pl.BlockSpec((1, width), lambda i, info: (0, 0))],
            out_specs=[
                rows_of(width),
                rows_of(width),
                pl.BlockSpec((width, tile), lambda i, info: (0, i)),
                pl.BlockSpec((4, tile, feats), lambda i, info: (0, i, 0)),
            ],
            scratch_shapes=[pltpu.VMEM((4, width, feats), BF16), pltpu.SemaphoreType.DMA],
        ),
        out_shape=[
            shape_of((tok, width), F32),
            shape_of((tok, width), BF16),
            shape_of((width, tok), BF16),
            shape_of((4, tok, feats), BF16),
        ],
        compiler_params=settings(1, 60),
        cost_estimate=cost(True),
        name="out_proj",
    )(info, *pieces, x, *mine, *theirs, gain)


def norm_two_back_kernel(plan, count, info, *refs):
    g_ref, r_ref, gr_ref, gain_ref, gres_ref, gat_ref, a0, a1, b0, b1, gg_ref, w_ref, sem = refs[count:]
    load_blocks(plan, refs, w_ref, sem)
    ctx = info[2]
    grad, resid = g_ref[...], r_ref[...]
    rho = lax.rsqrt(jnp.mean(resid * resid, axis=-1, keepdims=True) + EPS)
    unit = resid * rho
    scaled = grad * gain_ref[...]
    back = rho * (scaled - unit * jnp.mean(scaled * unit, axis=-1, keepdims=True))
    total = gr_ref[...] + back
    gres_ref[...] = total
    low = total.astype(BF16)
    gat_ref[...] = total.T.astype(BF16)

    @pl.when(pl.program_id(0) == 0)
    def _():
        gg_ref[...] = jnp.zeros_like(gg_ref)

    gg_ref[...] += jnp.sum(grad * unit, axis=0, keepdims=True)
    for j, ref, side in ((0, a0, ctx), (1, a1, ctx), (0, b0, 1 - ctx), (1, b1, 1 - ctx)):
        ref[...] = dot(low, w_ref[2 * side + j], 1, 0).astype(BF16)


def norm_two_back(info, grad, resid, grad_result, gain, weights, tile):
    plan, pieces = weights
    tok, width = grad.shape
    feats = pieces[0].shape[1]
    rows_of = lambda n: pl.BlockSpec((tile, n), lambda i, info: (i, 0))
    row = pl.BlockSpec((1, width), lambda i, info: (0, 0))
    return pl.pallas_call(
        functools.partial(norm_two_back_kernel, plan, len(pieces)),
        grid_spec=pltpu.PrefetchScalarGridSpec(
            num_scalar_prefetch=1,
            grid=(tok // tile,),
            in_specs=[ANY] * len(pieces) + [rows_of(width)] * 3 + [row],
            out_specs=[rows_of(width), pl.BlockSpec((width, tile), lambda i, info: (0, i))]
            + [rows_of(feats)] * 4
            + [row],
            scratch_shapes=[pltpu.VMEM((4, width, feats), BF16), pltpu.SemaphoreType.DMA],
        ),
        out_shape=[shape_of((tok, width), F32), shape_of((width, tok), BF16)]
        + [shape_of((tok, feats), BF16)] * 4
        + [shape_of((1, width), F32)],
        compiler_params=settings(1, 60),
        cost_estimate=cost(True),
        name="norm_two_back",
    )(info, *pieces, grad, resid, grad_result, gain)


def norm_one_back_kernel(plan, count, info, *refs):
    p0, p1, x_ref, gres_ref, gain_ref, *out_refs, gg_ref, w_ref, sem = refs[count:]
    load_blocks(plan, refs, w_ref, sem)
    quarter = x_ref.shape[1] // 4
    grad = dot(p0[0], w_ref[0], 1, 1)
    grad = grad + dot(p1[0], w_ref[1], 1, 1)
    grad = grad + dot(p0[1], w_ref[2], 1, 1)
    grad = grad + dot(p1[1], w_ref[3], 1, 1)
    x = x_ref[...].astype(F32)
    rho = lax.rsqrt(jnp.mean(x * x, axis=-1, keepdims=True) + EPS)
    unit = x * rho
    scaled = grad * gain_ref[...]
    back = rho * (scaled - unit * jnp.mean(scaled * unit, axis=-1, keepdims=True))
    total = (gres_ref[...] + back).astype(BF16)
    for p, mask in enumerate(MASKS):
        at = pl.multiple_of(jnp.bitwise_xor(info[1], mask) * quarter, quarter)
        part = total[:, p * quarter : (p + 1) * quarter]

        for i, out_ref in enumerate(out_refs):

            @pl.when(pl.program_id(0) == i)
            def _():
                out_ref[:, pl.ds(at, quarter)] = part

    @pl.when(pl.program_id(0) == 0)
    def _():
        gg_ref[...] = jnp.zeros_like(gg_ref)

    gg_ref[...] += jnp.sum(grad * unit, axis=0, keepdims=True)


def norm_one_back(info, pairs, weights, x, grad_resid, gain, tile):
    plan, pieces = weights
    tok, width = x.shape
    cols = pieces[0].shape[1]
    rows_of = lambda n: pl.BlockSpec((tile, n), lambda i, info: (i, 0))
    pair = pl.BlockSpec((2, tile, cols), lambda i, info: (0, i, 0))
    row = pl.BlockSpec((1, width), lambda i, info: (0, 0))
    return pl.pallas_call(
        functools.partial(norm_one_back_kernel, plan, len(pieces)),
        grid_spec=pltpu.PrefetchScalarGridSpec(
            num_scalar_prefetch=1,
            grid=(tok // tile,),
            in_specs=[ANY] * len(pieces) + [pair, pair, rows_of(width), rows_of(width), row],
            out_specs=[pl.BlockSpec((tile, width), lambda i, info: (0, 0))] * 4 + [row],
            scratch_shapes=[pltpu.VMEM((4, width, cols), BF16), pltpu.SemaphoreType.DMA],
        ),
        out_shape=[shape_of((tile, width), BF16)] * 4 + [shape_of((1, width), F32)],
        compiler_params=settings(1, 60),
        cost_estimate=cost(True),
        name="norm_one_back",
    )(info, *pieces, *pairs, x, grad_resid, gain)


def weight_copies(plan, pieces, gate_up, down, gate_up_sem, down_sem):
    third = down.shape[1] // 3
    rows = down.shape[0] // 4
    wide, thin = [], []
    for p, chunks in enumerate(plan):
        block = pl.ds(p * rows, rows)
        for j, (piece, row, at) in enumerate(chunks):
            src = pieces[piece].at[pl.ds(row, rows)]
            wide.append(
                pltpu.make_async_copy(
                    src.at[:, pl.ds(at, 2 * third)],
                    gate_up.at[block, pl.ds(j * 2 * third, 2 * third)],
                    gate_up_sem,
                )
            )
            thin.append(
                pltpu.make_async_copy(
                    src.at[:, pl.ds(at + 2 * third, third)],
                    down.at[block, pl.ds(j * third, third)],
                    down_sem,
                )
            )
    return wide, thin


def split_act(act):
    third = act.shape[1] // 6
    part = lambda j: act[:, j * third : (j + 1) * third]
    return [(part(0), part(1)), (part(2), part(3)), (part(4), part(5))]


def ffn_fwd_kernel(tile, plans, last, info, scale, x_ref, in_ref, *rest):
    if last:
        teach_ref, rest = rest[0], rest[1:]
    pieces = []
    for plan in plans:
        count = 1 + max(place[0] for chunks in plan for place in chunks)
        pieces.append(rest[:count])
        rest = rest[count:]
    act_ref, hid_ref = rest[:2]
    if last:
        outa_ref, outb_ref, gres_ref, low_ref, lowt_ref, sq_ref = rest[2:8]
        gate_up, down, total, sems = rest[8:]
    else:
        sum_ref, gate_up, down, total, sems = rest[2:]
    step, part = pl.program_id(0), pl.program_id(1)
    final = len(plans) - 1
    width = x_ref.shape[1]
    quarter = width // 4
    third = down.shape[2] // 3

    def copies(s):
        return weight_copies(
            plans[s], pieces[s], gate_up.at[s], down.at[s], sems.at[s, 0], sems.at[s, 1]
        )

    @pl.when((step == 0) & (part == 0))
    def _():
        for s in range(len(plans)):
            wide, thin = copies(s)
            for copy in wide + thin:
                copy.start()

    for s in range(len(plans)):

        @pl.when((step == s) & (part == 0))
        def _():
            pltpu.make_async_copy(gate_up.at[s], gate_up.at[s], sems.at[s, 0]).wait()

    rows = pl.ds(pl.multiple_of(part * tile, tile), tile)
    act = dot(x_ref[rows, :], gate_up[step], 1, 0)
    for j, (gate, upper) in enumerate(split_act(act)):
        sig = sigmoid(gate)
        silu = gate * sig
        hid_ref[0, :, j * third : (j + 1) * third] = (silu * upper).astype(BF16)
        at = 2 * j * third
        act_ref[0, :, at : at + third] = (upper * (sig + silu - silu * sig)).astype(BF16)
        act_ref[0, :, at + third : at + 2 * third] = silu.astype(BF16)
    for s in range(len(plans)):

        @pl.when((step == s) & (part == 0))
        def _():
            pltpu.make_async_copy(down.at[s], down.at[s], sems.at[s, 1]).wait()

    grown = dot(hid_ref[0], down[step], 1, 1)

    @pl.when(step == 0)
    def _():
        total[rows, :] = in_ref[...] + grown

    @pl.when(step > 0)
    def _():
        total[rows, :] += grown

    @pl.when(step == final)
    def _():
        result = total[rows, :]
        if not last:
            sum_ref[...] = result
            return
        tok = x_ref.shape[0]
        slot = info[2] * tok + part * tile + lax.broadcasted_iota(jnp.int32, (tile, 1), 0)
        valid = jnp.where(slot < info[3], 1.0, 0.0)
        square = jnp.zeros((tile, quarter), F32)
        for p, mask in enumerate(MASKS):
            at = pl.multiple_of(jnp.bitwise_xor(info[1], mask) * quarter, quarter)
            cols = slice(p * quarter, (p + 1) * quarter)
            value = result[:, cols]
            low = value.astype(BF16)

            @pl.when(part < pl.num_programs(1) // 2)
            def _():
                outa_ref[:, pl.ds(at, quarter)] = low

            @pl.when(part >= pl.num_programs(1) // 2)
            def _():
                outb_ref[:, pl.ds(at, quarter)] = low

            error = valid * (value - teach_ref[0, :, pl.ds(at, quarter)].astype(F32))
            square = square + error * error
            grad = error * scale[0]
            gres_ref[:, cols] = grad
            low_ref[:, cols] = grad.astype(BF16)
            lowt_ref[cols, :] = grad.T.astype(BF16)

        @pl.when(part == 0)
        def _():
            sq_ref[...] = jnp.zeros_like(sq_ref)

        sq_ref[...] += jnp.sum(square, axis=0, keepdims=True)


def ffn_fwd(info, scale, x, total, teacher, weights, units, tile):
    tok, width = x.shape
    pieces = [piece for _, group in weights for piece in group]
    count = len(weights)
    last = teacher is not None
    entry = lambda s, i: jnp.where(s == 0, i, tok // tile - 1)
    leave = lambda s, i: jnp.where(s == count - 1, i, 0)
    tiles = lambda n: pl.BlockSpec((tile, n), lambda s, i, info: (leave(s, i), 0))
    slab = lambda n: pl.BlockSpec((1, tile, n), lambda s, i, info: (s, i, 0))
    in_specs = [
        SMEM,
        whole((tok, width)),
        pl.BlockSpec((tile, width), lambda s, i, info: (entry(s, i), 0)),
    ]
    out_specs = [slab(2 * units), slab(units)]
    out_shape = [shape_of((count, tok, 2 * units), BF16), shape_of((count, tok, units), BF16)]
    if last:
        in_specs.append(
            pl.BlockSpec((1, tile, width), lambda s, i, info: (info[0], leave(s, i), 0))
        )
        half = tok // tile // 2
        out_specs += [
            pl.BlockSpec(
                (tile, width), lambda s, i, info: (jnp.minimum(leave(s, i), half - 1), 0)
            ),
            pl.BlockSpec(
                (tile, width), lambda s, i, info: (jnp.maximum(leave(s, i) - half, 0), 0)
            ),
            tiles(width),
            tiles(width),
            pl.BlockSpec((width, tile), lambda s, i, info: (0, leave(s, i))),
            pl.BlockSpec((1, width // 4), lambda s, i, info: (0, 0)),
        ]
        out_shape += [
            shape_of((tok // 2, width), BF16),
            shape_of((tok // 2, width), BF16),
            shape_of((tok, width), F32),
            shape_of((tok, width), BF16),
            shape_of((width, tok), BF16),
            shape_of((1, width // 4), F32),
        ]
    else:
        out_specs.append(tiles(width))
        out_shape.append(shape_of((tok, width), F32))
    return pl.pallas_call(
        functools.partial(ffn_fwd_kernel, tile, [plan for plan, _ in weights], last),
        grid_spec=pltpu.PrefetchScalarGridSpec(
            num_scalar_prefetch=1,
            grid=(count, tok // tile),
            in_specs=in_specs + [ANY] * len(pieces),
            out_specs=out_specs,
            scratch_shapes=[
                pltpu.VMEM((count, width, 2 * units), BF16),
                pltpu.VMEM((count, width, units), BF16),
                pltpu.VMEM((tok, width), F32),
                pltpu.SemaphoreType.DMA((count, 2)),
            ],
        ),
        out_shape=out_shape,
        compiler_params=settings(2, 60),
        cost_estimate=cost(True),
        name="ffn_fwd",
    )(info, scale, x, total, *([teacher] if last else []), *pieces)


def ffn_bwd_kernel(steps, plan, first, low_ref, act_ref, hid_ref, xt_ref, lowt_ref, *rest):
    count = 1 + max(place[0] for chunks in plan for place in chunks)
    pieces, rest = rest[:count], rest[count:]
    if not first:
        in_ref, rest = rest[0], rest[1:]
    out_ref, keep_ref, send_ref, gate_up, down, dact_all, hid_all, sems = rest
    step = pl.program_id(0)
    units = down.shape[1]
    third = units // 3
    tile = low_ref.shape[0]

    @pl.when(step == 0)
    def _():
        wide, thin = weight_copies(plan, pieces, gate_up, down, sems.at[0], sems.at[1])
        for copy in thin + wide:
            copy.start()
        pltpu.make_async_copy(down, down, sems.at[1]).wait()

    @pl.when(step < steps)
    def _():
        rows = pl.ds(pl.multiple_of(step * tile, tile), tile)
        grad_hidden = dot(low_ref[...], down[...], 1, 0)
        for j, (to_gate, to_upper) in enumerate(split_act(act_ref[0])):
            grad = grad_hidden[:, j * third : (j + 1) * third]
            at = 2 * j * third
            dact_all[rows, at : at + third] = (grad * to_gate.astype(F32)).astype(BF16)
            dact_all[rows, at + third : at + 2 * third] = (grad * to_upper.astype(F32)).astype(BF16)
        hid_all[rows, :] = hid_ref[0]

        @pl.when(step == 0)
        def _():
            pltpu.make_async_copy(gate_up, gate_up, sems.at[0]).wait()

        grown = dot(dact_all[rows, :], gate_up[...], 1, 1)
        out_ref[...] = grown if first else in_ref[...] + grown

    def weight_rows(target):
        target[:, : 2 * units] = dot(xt_ref[...], dact_all[...], 1, 0).astype(BF16)
        target[:, 2 * units :] = dot(lowt_ref[...], hid_all[...], 1, 0).astype(BF16)

    @pl.when((step >= steps) & (step < steps + 2))
    def _():
        weight_rows(send_ref)

    @pl.when(step >= steps + 2)
    def _():
        weight_rows(keep_ref)


def ffn_bwd(low, saved, weights, total, xt, lowt, tile):
    plan, pieces = weights
    acts, hiddens, block = saved
    tok, width = low.shape
    units = hiddens.shape[2]
    steps = tok // tile
    quarter = width // 4
    first = total is None
    clip = lambda i: jnp.minimum(i, steps - 1)
    rows_of = lambda n: pl.BlockSpec((tile, n), lambda i: (clip(i), 0))
    slab = lambda n: pl.BlockSpec((1, tile, n), lambda i: (block, clip(i), 0))
    feature = lambda i: (jnp.where(i < steps + 2, jnp.maximum(i - steps, 0) + 2, i - steps - 2), 0)
    return pl.pallas_call(
        functools.partial(ffn_bwd_kernel, steps, plan, first),
        grid=(steps + 4,),
        in_specs=[
            rows_of(width),
            slab(2 * units),
            slab(units),
            pl.BlockSpec((quarter, tok), feature),
            pl.BlockSpec((quarter, tok), feature),
        ]
        + [ANY] * len(pieces)
        + ([] if first else [rows_of(width)]),
        out_specs=[
            rows_of(width),
            pl.BlockSpec((quarter, 3 * units), lambda i: (jnp.maximum(i - steps - 2, 0), 0)),
            pl.BlockSpec((quarter, 3 * units), lambda i: (jnp.clip(i - steps, 0, 1), 0)),
        ],
        out_shape=[
            shape_of((tok, width), F32),
            shape_of((width // 2, 3 * units), BF16),
            shape_of((width // 2, 3 * units), BF16),
        ],
        scratch_shapes=[
            pltpu.VMEM((width, 2 * units), BF16),
            pltpu.VMEM((width, units), BF16),
            pltpu.VMEM((tok, 2 * units), BF16),
            pltpu.VMEM((tok, units), BF16),
            pltpu.SemaphoreType.DMA((2,)),
        ],
        input_output_aliases={} if first else {5 + len(pieces): 0},
        compiler_params=settings(1, 60),
        cost_estimate=cost(True),
        name="ffn_bwd",
    )(low, acts, hiddens, xt, lowt, *pieces, *([] if first else [total]))


def turn_chunks(block):
    wide = block.shape[1] * 2 // 9
    thin = wide // 2
    starts = [(2 * wide, wide), (wide, wide), (0, wide)]
    starts += [(3 * wide + 2 * thin, thin), (3 * wide + thin, thin), (3 * wide, thin)]
    return jnp.concatenate([block[:, a : a + n] for a, n in starts], axis=1)


def sum_kernel(turns, *refs):
    total = None
    for ref, turn in zip(refs[:-1], turns):
        value = ref[...].astype(F32)
        value = turn_chunks(value) if turn else value
        total = value if total is None else total + value
    refs[-1][...] = total.astype(refs[-1].dtype)


def summed(terms, turns=None, dtype=BF16):
    rows, cols = terms[0].shape
    spec = pl.BlockSpec((128, cols), lambda i: (i, 0))
    return pl.pallas_call(
        functools.partial(sum_kernel, turns or [False] * len(terms)),
        grid=(rows // 128,),
        in_specs=[spec] * len(terms),
        out_specs=spec,
        out_shape=shape_of((rows, cols), dtype),
        compiler_params=settings(1, 60),
        cost_estimate=cost(False),
        name="summed",
    )(*terms)


def sums_kernel(jobs, count, info, *refs):
    arrays, refs = refs[:count], refs[count:]
    outs, (term_buf, out_buf, term_sems, out_sems) = refs[: len(jobs)], refs[len(jobs) :]
    rows = term_buf.shape[1]
    copies = []
    for terms in jobs:
        group = []
        for array, base, pick, _ in terms:
            at = base
            if pick is not None:
                at = pl.multiple_of(base + jnp.bitwise_xor(info[2], pick) * rows, rows)
            i = len(copies) + len(group)
            src = arrays[array].at[pl.ds(at, rows)]
            group.append(pltpu.make_async_copy(src, term_buf.at[i], term_sems.at[i]))
            group[-1].start()
        copies += group
    first = 0
    stores = []
    for j, terms in enumerate(jobs):
        total = None
        for i, (_, _, _, turn) in enumerate(terms):
            copies[first + i].wait()
            value = term_buf[first + i].astype(F32)
            value = turn_chunks(value) if turn else value
            total = value if total is None else total + value
        first += len(terms)
        out_buf[j] = total.astype(BF16)
        stores.append(pltpu.make_async_copy(out_buf.at[j], outs[j], out_sems.at[j]))
        stores[-1].start()
    for store in stores:
        store.wait()


def sums(info, arrays, jobs):
    cols = arrays[0].shape[1]
    rows, terms = 128, sum(len(job) for job in jobs)
    return pl.pallas_call(
        functools.partial(sums_kernel, jobs, len(arrays)),
        grid_spec=pltpu.PrefetchScalarGridSpec(
            num_scalar_prefetch=1,
            grid=(1,),
            in_specs=[ANY] * len(arrays),
            out_specs=[ANY] * len(jobs),
            scratch_shapes=[
                pltpu.VMEM((terms, rows, cols), BF16),
                pltpu.VMEM((len(jobs), rows, cols), BF16),
                pltpu.SemaphoreType.DMA((terms,)),
                pltpu.SemaphoreType.DMA((len(jobs),)),
            ],
        ),
        out_shape=[shape_of((rows, cols), BF16)] * len(jobs),
        compiler_params=settings(1, 60),
        cost_estimate=cost(False),
        name="sums",
    )(info, *arrays)


def core_jobs(keep, came):
    return [[(a, far * 256, pick, False) for a in (keep, came)] for far in (0, 1) for pick in (0, 1)]


def core_sum_kernel(info, left_ref, right_ref, *outs):
    total = (left_ref[...].astype(F32) + right_ref[...].astype(F32)).astype(BF16)
    block = pl.program_id(1)
    place = block // 2 * 2 + jnp.bitwise_xor(block % 2, info[2])
    for i, out in enumerate(outs):

        @pl.when(place == i)
        def _():
            out[...] = total


def core_sum(info, keep, came):
    groups, rows, cols = keep.shape
    spec = pl.BlockSpec((1, rows // 4, cols), lambda g, i, info: (g, i, 0))
    return pl.pallas_call(
        core_sum_kernel,
        grid_spec=pltpu.PrefetchScalarGridSpec(
            num_scalar_prefetch=1,
            grid=(groups, 4),
            in_specs=[spec] * 2,
            out_specs=[pl.BlockSpec((1, rows // 4, cols), lambda g, i, info: (g, 0, 0))] * 4,
        ),
        out_shape=[shape_of((groups, rows // 4, cols), BF16)] * 4,
        compiler_params=settings(2, 24),
        cost_estimate=cost(False),
        name="core_sum",
    )(info, keep, came)


def weight_grad_kernel(nt_ref, back0_ref, back1_ref, gt_ref, att_ref, keep_ref, send_ref):
    cols = back0_ref.shape[2]
    part, block = pl.program_id(0), pl.program_id(1)

    def rows(target, back_ref):
        target[0, :, :cols] = dot(nt_ref[...], back_ref[0], 1, 0).astype(BF16)
        target[0, :, cols:] = dot(gt_ref[...], att_ref[0], 1, 0).astype(BF16)

    for j, back_ref in enumerate((back0_ref, back1_ref)):

        @pl.when((part == 0) & (block % 2 == j))
        def _():
            rows(send_ref, back_ref)

        @pl.when((part == 1) & (block % 2 == j))
        def _():
            rows(keep_ref, back_ref)


def weight_grad(normed_t, backs, grad_t, attended):
    width, tok = normed_t.shape
    cols, feats = backs[0].shape[2], attended.shape[2]
    half = pl.BlockSpec((width // 2, tok), lambda p, k: (1 - p, 0))
    side = pl.BlockSpec((1, tok, cols), lambda p, k: (k // 2, 0, 0))
    shape = (1, width // 2, cols + feats)
    return pl.pallas_call(
        weight_grad_kernel,
        grid=(2, 4),
        in_specs=[half, side, side, half, pl.BlockSpec((1, tok, feats), lambda p, k: (k, 0, 0))],
        out_specs=[
            pl.BlockSpec(shape, lambda p, k: (jnp.where(p == 0, 0, k), 0, 0)),
            pl.BlockSpec(shape, lambda p, k: (jnp.where(p == 0, k, 3), 0, 0)),
        ],
        out_shape=[shape_of((4, width // 2, cols + feats), BF16)] * 2,
        compiler_params=settings(2, 60),
        cost_estimate=cost(True),
        name="weight_grad",
    )(normed_t, *backs, grad_t, attended)


def after(value, *others):
    return lax.optimization_barrier((value,) + others)[0]


def per_device_rows(
    tokens,
    teacher,
    lengths,
    attn_gain,
    q_weight,
    k_weight,
    v_weight,
    q_gain,
    k_gain,
    o_weight,
    ffn_gain,
    gate_weight,
    up_weight,
    down_weight,
):
    z = lax.axis_index("tp")
    ctx = lax.axis_index("ctx")
    fsdp = lax.axis_index("fsdp")
    rows_dev, tok, width = tokens.shape
    quarter = width // 4
    hd = q_gain.shape[0] * 4
    q_cols, k_cols = q_weight.shape[1], k_weight.shape[1]
    proj = q_cols + 2 * k_cols
    heads = (q_cols // hd, k_cols // hd)
    units = gate_weight.shape[1]
    slots = rows_dev * 4 * tok * 2

    def x_swap(v):
        return lax.ppermute(v, "fsdp", X_SWAP)

    def core_swap(v):
        return lax.ppermute(v, "fsdp", CORE_SWAP)

    def y_swap(v):
        return lax.ppermute(v, "ctx", Y_SWAP)

    def z_up(v):
        return lax.ppermute(v, "tp", Z_UP)

    def z_far(v):
        return lax.ppermute(v, "tp", Z_FAR)

    def z_down(v):
        return lax.ppermute(v, "tp", Z_DOWN)

    def natural(v):
        v = jnp.concatenate([v[0:1], v[2:3], v[1:2], v[3:4]], axis=0)
        v = jnp.where(fsdp % 2 == 0, v, jnp.concatenate([v[1:2], v[0:1], v[3:4], v[2:3]], axis=0))
        return jnp.where(fsdp // 2 == 0, v, jnp.concatenate([v[2:4], v[0:2]], axis=0))

    v = {}

    def sync():
        v.update(lax.optimization_barrier(dict(v)))

    length = lax.dynamic_slice_in_dim(lengths, z, 1, 0)
    info = jnp.concatenate([jnp.stack([z, fsdp, ctx]).astype(jnp.int32), length])
    w_proj = join(q_weight, k_weight, v_weight)
    proj_z = [z_up(w_proj), z_far(w_proj), z_down(w_proj)]
    proj_z[2] = after(proj_z[2], proj_z[0])
    proj_z[1] = after(proj_z[1], proj_z[2])
    proj_zfar = [x_swap(block) for block in proj_z]
    proj_own = jnp.concatenate([w_proj, x_swap(w_proj)], axis=0)
    count_here = jnp.sum(lengths).astype(F32)[None]
    vector = jnp.concatenate([attn_gain, ffn_gain, q_gain, k_gain]).astype(F32)
    vector = jnp.concatenate([vector, count_here, jnp.zeros((640 - 545,), F32)])[None]
    vector = jnp.concatenate([vector, x_swap(vector)], axis=0)
    vector = jnp.concatenate([vector, core_swap(vector)], axis=0)
    w_out, w_ffn, *w_chunks = pack(info, o_weight, gate_weight, up_weight, down_weight)
    pos = (ctx * tok + jnp.arange(tok, dtype=jnp.int32)).astype(F32)
    frequency = THETA ** (-(2.0 * jnp.arange(hd // 2, dtype=F32)) / hd)
    angles = frequency[:, None] * pos[None, :]
    head_gains = natural(vector[:, 2 * quarter : 544])
    gain_one = vector[:, :quarter].reshape(1, width)
    x_in, normed_one_t = norm_one(info, tokens, gain_one, 256)
    out_start = after(w_out, proj_z[1])
    out_z = [z_up(out_start), z_far(out_start), z_down(out_start)]
    v.update(
        info=info,
        proj_own=proj_own,
        proj_z=jnp.concatenate(proj_z, axis=0),
        proj_zfar=proj_zfar,
        own_core=core_swap(proj_own),
        w_out=w_out,
        out_z=out_z,
        w_ffn=w_ffn,
        w_chunks=w_chunks,
        x_in=x_in,
        normed_one_t=normed_one_t,
        gain_one=gain_one,
        gain_two=vector[:, quarter : 2 * quarter].reshape(1, width),
        total_count=jnp.sum(vector[:, 544]),
        gain_q=head_gains[:, : hd // 4].reshape(hd, 1),
        gain_k=head_gains[:, hd // 4 :].reshape(hd, 1),
        cos_part=jnp.cos(angles),
        sin_part=jnp.sin(angles),
    )
    sync()
    info = v["info"]

    plan_proj = [[(0, 0), (0, quarter), (5, 0), (5, quarter)]]
    plan_proj += [[(1, k * quarter), (2 + k, 0), (6, k * quarter), (7 + k, 0)] for k in range(3)]
    weights_proj = [v["proj_own"], v["proj_z"]] + v["proj_zfar"] + [v["own_core"]]
    weights_proj += [core_swap(part) for part in [v["proj_z"]] + v["proj_zfar"]]
    one = [z_up(v["w_chunks"][0]), z_up(v["w_chunks"][3])]
    ffn_far = x_swap(v["w_ffn"])
    tables = [v[name] for name in ("cos_part", "sin_part", "gain_q", "gain_k")]

    def make(block, *then):
        normed_t = after(v["normed_one_t"], *then)
        return project(info, (plan_proj, weights_proj), normed_t, *tables, heads, block)

    theirs = [make(lambda s: 2 * (1 - s[2]))]
    got = [y_swap(theirs[0][0])]
    theirs.append(make(lambda s: 2 * (1 - s[2]) + 1, theirs[0][0]))
    got.append(y_swap(theirs[1][0]))
    mine = [make(lambda s: 2 * s[2], theirs[1][0])]
    mine.append(make(lambda s: 2 * s[2] + 1, mine[0][0]))
    v.update(
        one=one,
        ffn_far=ffn_far,
        weights_proj=weights_proj,
        mine=mine,
        theirs=theirs,
        got0=got[0],
    )
    sync()

    one_far = [x_swap(v["one"][0])]
    three = [z_down(v["w_chunks"][0])]
    own_cores = [core_swap(v["w_ffn"]), core_swap(v["ffn_far"])]
    first = attn_fwd(info, v["mine"][0][0], v["got0"], hd)
    v.update(first=first, got1=got[1], one_far=one_far, three=three, own_cores=own_cores)
    sync()

    arrived = [y_swap(v["first"][1])]
    three = v["three"] + [z_down(v["w_chunks"][1])]
    out_blocks = jnp.concatenate([v["w_out"]] + v["out_z"], axis=0)
    out_far = x_swap(out_blocks)
    one_cores = [core_swap(v["one"][0]), core_swap(v["one_far"][0])]
    second = attn_fwd(info, v["mine"][1][0], v["got1"], hd)
    v.update(
        second=second,
        arrived=arrived,
        three=three,
        out_blocks=out_blocks,
        out_far=out_far,
        one_cores=one_cores,
    )
    sync()

    arrived = v["arrived"] + [y_swap(v["second"][1])]
    three = v["three"] + [z_down(v["w_chunks"][2])]
    one_far = v["one_far"] + [x_swap(v["one"][1][:, :units])]
    weights_out = [v["out_blocks"], v["out_far"]]
    weights_out += [core_swap(v["out_blocks"]), core_swap(v["out_far"])]
    v.update(arrived=arrived, three=three, one_far=one_far, weights_out=weights_out)
    sync()

    plan_out = [[(p, k * quarter) for p in range(4)] for k in range(4)]
    two = [z_up(v["one"][0])]
    three_far = [x_swap(v["three"][0])]
    one_far = v["one_far"] + [y_swap(v["one_far"][0])]
    one_cores = v["one_cores"] + [core_swap(v["one"][1]), core_swap(v["one_far"][1])]
    resid, normed_two, normed_two_t, attended = out_proj(
        info,
        v["x_in"],
        [v["first"][0], v["second"][0]],
        v["arrived"],
        (plan_out, v["weights_out"]),
        v["gain_two"],
        256,
    )
    v.update(
        two=two,
        three_far=three_far,
        one_far=one_far,
        one_cores=one_cores,
        resid=resid,
        normed_two=normed_two,
        normed_two_t=normed_two_t,
        attended=attended,
    )
    sync()

    plan0 = [[(i, 0, j * units) for j in range(3)] for i in range(4)]
    plan_mixed = [[(0, 0, 0), (1, 0, 0), (1, 0, units)], [(i, 0, 0) for i in (2, 3, 4)]]
    plan_mixed += [[(5, 0, 0), (6, 0, 0), (6, 0, units)], [(i, 0, 0) for i in (7, 8, 9)]]
    scale = (slots / v["total_count"])[None]
    weights0 = [v["w_ffn"], v["ffn_far"]] + v["own_cores"]
    c0, cf, c1, cb = v["one_cores"]
    weights1 = v["one"] + v["one_far"] + [c0, c1, cf, cb, core_swap(v["one_far"][2])]
    two = v["two"] + [z_up(v["one"][1])]
    three_far = v["three_far"] + [x_swap(v["three"][1]), y_swap(v["three_far"][0])]
    two_far = [x_swap(v["two"][0])]
    three_cores = [core_swap(v["three"][0])]
    acts_a, hiddens_a, sum_a = ffn_fwd(
        info,
        scale,
        v["normed_two"],
        v["resid"],
        None,
        [(plan0, weights0), (plan_mixed, weights1)],
        units,
        256,
    )
    v.update(
        scale=scale,
        weights0=weights0,
        weights1=weights1,
        two=two,
        three_far=three_far,
        two_far=two_far,
        three_cores=three_cores,
        acts_a=acts_a,
        hiddens_a=hiddens_a,
        sum_a=sum_a,
    )
    sync()

    plan_chunks = [[(3 * p + j, 0, 0) for j in range(3)] for p in range(4)]
    weights3 = v["three"] + v["three_far"] + v["three_cores"]
    weights3 += [core_swap(part) for part in v["three"][1:]]
    weights3 += [core_swap(part) for part in v["three_far"]]
    two_far = v["two_far"] + [x_swap(v["two"][1][:, :units]), y_swap(v["two_far"][0])]
    two_cores = [core_swap(part) for part in v["two"] + v["two_far"]]
    acts_b, hiddens_b, sum_b = ffn_fwd(
        info, v["scale"], v["normed_two"], v["sum_a"], None, [(plan_chunks, weights3)], units, 256
    )
    v.update(
        weights3=weights3,
        two_far=two_far,
        two_cores=two_cores,
        acts_b=acts_b,
        hiddens_b=hiddens_b,
        sum_b=sum_b,
    )
    sync()

    weights2 = v["two"] + v["two_far"] + v["two_cores"]
    weights2 += [core_swap(part) for part in v["two_far"][1:]]
    acts_c, hiddens_c, *results, grad_result, grad_low, grad_low_t, square = ffn_fwd(
        info, v["scale"], v["normed_two"], v["sum_b"], teacher, [(plan_mixed, weights2)], units, 256
    )
    v.update(
        weights2=weights2,
        acts_c=acts_c,
        hiddens_c=hiddens_c,
        results=results,
        grad_result=grad_result,
        grad_low=grad_low,
        grad_low_t=grad_low_t,
        square=square,
    )
    sync()

    def ffn_back(plan, weights, acts, hiddens, block, total):
        return ffn_bwd(
            v["grad_low"],
            (v[acts], v[hiddens], block),
            (plan, v[weights]),
            total,
            v["normed_two_t"],
            v["grad_low_t"],
            256,
        )

    turned = [False, False, True]
    one = [z_up(v["results"][0])]
    total, keep2, send2 = ffn_back(plan_mixed, "weights2", "acts_c", "hiddens_c", 0, None)
    v.update(one=one, total=total, keep2=keep2, send2=send2)
    sync()

    one = v["one"] + [z_up(v["results"][1])]
    came2 = core_swap(v["send2"])
    total, keep1, send1 = ffn_back(plan_mixed, "weights1", "acts_a", "hiddens_a", 1, v["total"])
    v.update(one=one, came2=came2, total=total, keep1=keep1, send1=send1)
    sync()

    out_three = [z_down(v["results"][0])]
    came1 = core_swap(v["send1"])
    sum2 = sums(info, [v["keep2"], v["came2"]], core_jobs(0, 1))
    far_t2 = x_swap(sum2[3])
    total, keep3, send3 = ffn_back(
        plan_chunks, "weights3", "acts_b", "hiddens_b", 0, after(v["total"], sum2[0])
    )
    v.update(
        out_three=out_three,
        came1=came1,
        sum2=sum2,
        far_t2=far_t2,
        total=total,
        keep3=keep3,
        send3=send3,
    )
    sync()

    out_three = v["out_three"] + [z_down(v["results"][1])]
    came3 = core_swap(v["send3"])
    far_h2 = x_swap(v["sum2"][2])
    there2, *sum1 = sums(
        info,
        [v["sum2"][1], v["far_t2"], v["keep1"], v["came1"]],
        [[(0, 0, None, False), (1, 0, None, False)]] + core_jobs(2, 3),
    )
    there2 = y_swap(there2)
    total, keep0, send0 = ffn_back(
        plan0, "weights0", "acts_a", "hiddens_a", 0, after(v["total"], sum1[0])
    )
    v.update(
        out_three=out_three,
        came3=came3,
        far_h2=far_h2,
        there2=there2,
        sum1=sum1,
        total=total,
        keep0=keep0,
        send0=send0,
    )
    sync()

    came0 = core_swap(v["send0"])
    far_t1 = x_swap(v["sum1"][3])
    plane = [(0, 0, None, False), (1, 0, None, False), (2, 0, None, True)]
    part2, *sum3 = sums(
        info,
        [v["sum2"][0], v["far_h2"], v["there2"], v["keep3"], v["came3"]],
        [plane] + core_jobs(3, 4),
    )
    down2 = z_down(part2)
    grad_resid, grad_attn_t, a0, a1, b0, b1, gain_two_sum = norm_two_back(
        info,
        after(v["total"], sum3[0]),
        v["resid"],
        v["grad_result"],
        v["gain_two"],
        (plan_out, v["weights_out"]),
        256,
    )
    grad_got = [y_swap(b0), y_swap(b1)]
    v.update(
        came0=came0,
        far_t1=far_t1,
        down2=down2,
        sum3=sum3,
        grad_resid=grad_resid,
        grad_attn_t=grad_attn_t,
        grad_mine=[a0, a1],
        gain_two_sum=gain_two_sum,
        grad_got0=grad_got[0],
    )
    sync()

    def attn_back(j, grad):
        out, got_ref = v["first" if j == 0 else "second"], v[f"got{j}"]
        return attn_bwd(
            info, v["mine"][j][0], got_ref, out[0], out[1], grad, v[f"grad_got{j}"], out[2], hd
        )

    two = [z_up(v["one"][0])]
    far_h1 = x_swap(v["sum1"][2])
    there1, *sum0 = sums(
        info,
        [v["sum1"][1], v["far_t1"], v["keep0"], v["came0"]],
        [[(0, 0, None, False), (1, 0, None, False)]] + core_jobs(2, 3),
    )
    there1 = y_swap(there1)
    far_t3 = x_swap(v["sum3"][3])
    back0 = attn_back(0, after(v["grad_mine"][0], sum0[0]))
    v.update(
        out_two=two,
        far_h1=far_h1,
        there1=there1,
        far_t3=far_t3,
        sum0=sum0,
        back0=back0,
        grad_got1=grad_got[1],
    )
    sync()

    two = v["out_two"] + [z_up(v["one"][1])]
    heads0 = y_swap(v["back0"][1])
    far_h3 = x_swap(v["sum3"][2])
    far_t0 = x_swap(v["sum0"][3])
    there3, two_down = sums(
        info,
        [v["sum3"][1], v["far_t3"], v["sum1"][0], v["far_h1"], v["there1"], v["down2"]],
        [
            [(0, 0, None, False), (1, 0, None, False)],
            [(2, 0, None, False), (3, 0, None, False), (4, 0, None, True), (5, 0, None, False)],
        ],
    )
    there3_got = y_swap(there3)
    two_down_got = z_down(two_down)
    back1 = attn_back(1, after(v["grad_mine"][1], there3, two_down))
    v.update(
        out_two=two, heads0=heads0, far_h3=far_h3, far_t0=far_t0, there3=there3_got, back1=back1
    )
    sync()

    heads1 = y_swap(v["back1"][1])
    far_h0 = x_swap(v["sum0"][2])
    part3, there0 = sums(
        info,
        [v["sum3"][0], v["far_h3"], v["there3"], v["sum0"][1], v["far_t0"]],
        [plane, [(3, 0, None, False), (4, 0, None, False)]],
    )
    up3 = z_up(part3)
    tables = [v[name] for name in ("cos_part", "sin_part", "gain_q", "gain_k")]
    head0 = head_back(
        info, v["back0"][0], v["heads0"], v["mine"][0][1], v["theirs"][0][1], *tables, heads
    )
    v.update(heads1=heads1, two_down=two_down_got, head0=head0, there0=there0)
    sync()

    there0 = y_swap(v["there0"])
    head1 = head_back(
        info, v["back1"][0], v["heads1"], v["mine"][1][1], v["theirs"][1][1], *tables, heads
    )
    *tokens_low, gain_one_sum = norm_one_back(
        info,
        [v["head0"][0], head1[0]],
        (plan_proj, v["weights_proj"]),
        v["x_in"],
        v["grad_resid"],
        v["gain_one"],
        tok // 4,
    )
    v.update(head1=head1, tokens_low=tokens_low, gain_one_sum=gain_one_sum, up3=up3)
    v.update(there0=there0, far_h0=far_h0)
    sync()

    def place(out, parts, k, first):
        row = lax.rem(z - k + 4, 4)
        for j, part in enumerate(parts):
            at = (first + j) * part.shape[0]
            out = lax.dynamic_update_slice(out, part.astype(out.dtype)[None], (row, at, 0))
        return out

    v.update(out_one=v["one"])
    quarters = v["tokens_low"]
    one = [z_up(quarters[0])]
    keep, send = weight_grad(
        v["normed_one_t"], [v["head0"][0], v["head1"][0]], v["grad_attn_t"], v["attended"]
    )
    gain_heads = v["head0"][1] + v["head1"][1]
    vector = jnp.concatenate(
        [
            natural(v["gain_one_sum"].reshape(4, quarter)).reshape(1, width),
            natural(v["gain_two_sum"].reshape(4, quarter)).reshape(1, width),
            gain_heads[:, 0].reshape(1, hd),
            gain_heads[:, 1].reshape(1, hd),
            jnp.sum(v["square"]).reshape(1, 1),
            jnp.zeros((1, 127), F32),
        ],
        axis=1,
    )
    vector = vector + core_swap(vector)
    v.update(one=one, keep=keep, send=send)
    v.update(vector=vector)
    sync()

    one = v["one"] + [z_up(v["tokens_low"][1])]
    rows = quarter // 2
    flat = lambda a: a.reshape(4 * rows, a.shape[-1])
    attn_sums = [flat(p) for p in core_sum(info, v["keep"], core_swap(v["send"]))]
    vector = v["vector"] + x_swap(v["vector"])
    v.update(one=one, sums=attn_sums, vector=vector)
    sync()

    one = v["one"] + [z_up(v["tokens_low"][2])]
    far_t = x_swap(v["sums"][3])
    part0 = summed([v["sum0"][0], v["far_h0"], v["there0"]], turned)
    ffn_sum = summed([part0, v["two_down"], v["up3"]], None, F32)
    vector = v["vector"] + y_swap(v["vector"])
    v.update(one=one, far_t=far_t, ffn_sum=ffn_sum, vector=vector)
    sync()

    one = v["one"] + [z_up(v["tokens_low"][3])]
    three = [z_down(v["tokens_low"][0])]
    far_h = x_swap(v["sums"][2])
    there = y_swap(summed([v["sums"][1], v["far_t"]]))
    output = jnp.zeros((rows_dev, tok, width), BF16)
    for k, parts in enumerate((v["results"], v["out_one"], v["out_two"], v["out_three"])):
        output = place(output, parts, k, 0)
    v.update(one=one, three=three, far_h=far_h, there=there, output=output)
    sync()

    three = v["three"] + [z_down(v["tokens_low"][1])]
    parts = summed([v["sums"][0], v["far_h"], v["there"]])
    parts = [parts[k * rows : (k + 1) * rows] for k in range(4)]
    parts = [parts[0], z_down(parts[1]), z_far(parts[2]), z_up(parts[3])]
    ffn_other = y_swap(v["ffn_sum"])
    grad = place(jnp.zeros((rows_dev, tok, width), F32), v["tokens_low"], 0, 0)
    v.update(three=three, parts=parts, grad=grad)
    sync()

    three = v["three"] + [z_down(part) for part in v["tokens_low"][2:]]
    two = [z_up(v["one"][0])]
    attn_sum = summed(v["parts"], None, F32)
    vector = v["vector"] + lax.ppermute(v["vector"], "tp", Z_NEAR)
    grad = place(v["grad"], v["one"], 1, 0)
    v.update(three=three, two=two, attn_sum=attn_sum, vector=vector, grad=grad)
    v.update(ffn_other=ffn_other)
    sync()

    def finish(own, other):
        return jnp.concatenate(
            [jnp.where(ctx == 0, own, other), jnp.where(ctx == 0, other, own)], axis=0
        )

    def columns(first):
        parts = [ffn_grad[:, first(j) : first(j) + third] for j in range(3)]
        return jnp.concatenate(
            [
                jnp.where(ctx == 0, parts[0], parts[2]),
                parts[1],
                jnp.where(ctx == 0, parts[2], parts[0]),
            ],
            axis=1,
        )

    two = v["two"] + [z_up(part) for part in v["one"][1:]]
    attn_other = y_swap(v["attn_sum"])
    vector = v["vector"] + lax.ppermute(v["vector"], "tp", Z_FAR)
    third = units // 3
    ffn_grad = finish(v["ffn_sum"], turn_chunks(v["ffn_other"]))
    grad_gate = columns(lambda j: 2 * j * third)
    grad_up = columns(lambda j: (2 * j + 1) * third)
    grad_down = columns(lambda j: 2 * units + j * third).T
    grad = place(v["grad"], v["three"], 3, 0)
    grad = place(grad, v["two"], 2, 0)
    v.update(vector=vector, grad=grad, attn_other=attn_other)
    v.update(grad_gate=grad_gate, grad_up=grad_up, grad_down=grad_down, two=two)
    sync()

    tokens_grad = place(v["grad"], v["two"][1:], 2, 1)
    output = v["output"]
    sums_all = v["vector"][0]

    attn_grad = finish(v["attn_sum"], v["attn_other"])
    teacher_loss = sums_all[2 * width + 2 * hd] / (v["total_count"] * width)

    def own_part(at, size):
        return lax.dynamic_slice_in_dim(sums_all, at + fsdp * (size // 4), size // 4, 0)

    return (
        output,
        teacher_loss,
        tokens_grad,
        own_part(0, width),
        attn_grad[:, :q_cols],
        attn_grad[:, q_cols : q_cols + k_cols],
        attn_grad[:, q_cols + k_cols : proj],
        own_part(2 * width, hd),
        own_part(2 * width + hd, hd),
        attn_grad[:, proj:].T,
        own_part(width, width),
        v["grad_gate"],
        v["grad_up"],
        v["grad_down"],
    )


def solution(mesh):
    return jax.shard_map(
        per_device_rows if fits(mesh) else per_device_any,
        mesh=mesh,
        in_specs=(
            P("fsdp", "ctx", None),
            P("fsdp", "ctx", None),
            P("fsdp"),
            P("fsdp"),
            P("fsdp", "tp"),
            P("fsdp", "tp"),
            P("fsdp", "tp"),
            P("fsdp"),
            P("fsdp"),
            P("tp", "fsdp"),
            P("fsdp"),
            P("fsdp", "tp"),
            P("fsdp", "tp"),
            P("tp", "fsdp"),
        ),
        out_specs=(
            P("fsdp", "ctx", None),
            P(),
            P("fsdp", "ctx", None),
            P("fsdp"),
            P("fsdp", "tp"),
            P("fsdp", "tp"),
            P("fsdp", "tp"),
            P("fsdp"),
            P("fsdp"),
            P("tp", "fsdp"),
            P("fsdp"),
            P("fsdp", "tp"),
            P("fsdp", "tp"),
            P("tp", "fsdp"),
        ),
        check_vma=False,
    )
```

```python
import functools
import math

import jax
import jax.numpy as jnp
from jax import lax
from jax.experimental import pallas as pl
from jax.experimental.pallas import tpu as pltpu
from jax.sharding import PartitionSpec as P

EPS = 1e-05
THETA = 1000000.0
NEGATIVE = -1e30


def rms_scale(field_in, gain_vec):
    return (
        field_in * lax.rsqrt(jnp.mean(field_in * field_in, axis=-1, keepdims=True) + EPS) * gain_vec
    )


def rotate(field_in, positions):
    half_dim = field_in.shape[-1] // 2
    frequency = THETA ** (-(2.0 * jnp.arange(half_dim, dtype=jnp.float32)) / field_in.shape[-1])
    angles = positions[:, None] * frequency[None, :]
    cos_part = jnp.cos(angles)[:, None, :]
    sin_part = jnp.sin(angles)[:, None, :]
    lower_half = field_in[..., :half_dim]
    upper_half = field_in[..., half_dim:]
    return jnp.concatenate(
        [
            lower_half * cos_part - upper_half * sin_part,
            upper_half * cos_part + lower_half * sin_part,
        ],
        axis=-1,
    )


def linear(left_mat, right_mat):
    return jnp.dot(left_mat, right_mat, preferred_element_type=jnp.float32)


def linear_left(left_mat, right_mat):
    return lax.dot_general(
        left_mat, right_mat, (((0,), (0,)), ((), ())), preferred_element_type=jnp.float32
    )


def linear_right(left_mat, right_mat):
    return lax.dot_general(
        left_mat, right_mat, (((1,), (1,)), ((), ())), preferred_element_type=jnp.float32
    )


def swiglu(gate_act, up_act):
    return jax.nn.silu(gate_act) * up_act


def per_device_any(
    tokens,
    teacher,
    lengths,
    attn_gain,
    q_weight,
    k_weight,
    v_weight,
    q_gain,
    k_gain,
    o_weight,
    ffn_gain,
    gate_weight,
    up_weight,
    down_weight,
):
    (
        gain_one,
        w_query,
        w_key,
        w_value,
        gain_query,
        gain_key,
        w_output,
        gain_two,
        w_gate,
        w_upper,
        w_down,
    ) = (
        lax.all_gather(attn_gain, "fsdp", axis=0, tiled=True),
        lax.all_gather(q_weight, "fsdp", axis=0, tiled=True),
        lax.all_gather(k_weight, "fsdp", axis=0, tiled=True),
        lax.all_gather(v_weight, "fsdp", axis=0, tiled=True),
        lax.all_gather(q_gain, "fsdp", axis=0, tiled=True),
        lax.all_gather(k_gain, "fsdp", axis=0, tiled=True),
        lax.all_gather(o_weight, "fsdp", axis=1, tiled=True),
        lax.all_gather(ffn_gain, "fsdp", axis=0, tiled=True),
        lax.all_gather(gate_weight, "fsdp", axis=0, tiled=True),
        lax.all_gather(up_weight, "fsdp", axis=0, tiled=True),
        lax.all_gather(down_weight, "fsdp", axis=1, tiled=True),
    )
    rows_dev, block_len, model_width = tokens.shape
    count_tok = rows_dev * block_len
    head_dim = gain_query.shape[0]
    q_heads = w_query.shape[1] // head_dim
    kv_heads = w_key.shape[1] // head_dim
    group_size = q_heads // kv_heads
    score_scale = head_dim ** (-0.5)
    row_len = block_len * lax.axis_size("ctx")
    key_block = math.gcd(row_len, 512)
    block_start = lax.axis_index("ctx") * block_len
    tiles_used = (block_start + block_len + key_block - 1) // key_block
    slot_pos = block_start + jnp.arange(block_len, dtype=jnp.int32)
    positions = slot_pos.astype(jnp.float32)
    valid = (slot_pos[None, :] < lengths[:, None]).astype(jnp.float32)
    slots = count_tok * lax.axis_size("fsdp") * lax.axis_size("ctx")
    gain_two_f = gain_two.astype(jnp.float32)
    gain_one_f = gain_one.astype(jnp.float32)
    inputs = tokens.astype(jnp.float32)
    normed_one, back_one = jax.vjp(rms_scale, inputs, gain_one_f)
    normed_low = normed_one.astype(jnp.bfloat16).reshape(count_tok, model_width)
    query_raw = linear(normed_low, w_query)
    key_raw = linear(normed_low, w_key)
    value_raw = linear(normed_low, w_value)

    def heads_post(raw_heads, gain_vec):
        shaped = raw_heads.reshape(rows_dev, block_len, -1, head_dim)
        return rotate(rms_scale(shaped, gain_vec), positions)

    query_rot, query_back = jax.vjp(heads_post, query_raw, gain_query.astype(jnp.float32))
    key_rot, key_back = jax.vjp(heads_post, key_raw, gain_key.astype(jnp.float32))
    queries = query_rot.astype(jnp.bfloat16).reshape(
        rows_dev, block_len, kv_heads, group_size, head_dim
    )
    key_rows = key_rot.astype(jnp.bfloat16).reshape(rows_dev, block_len, kv_heads * head_dim)
    values = value_raw.astype(jnp.bfloat16).reshape(rows_dev, block_len, kv_heads * head_dim)
    keys_all, values_all = (
        lax.all_gather(key_rows, "ctx", axis=1, tiled=True),
        lax.all_gather(values, "ctx", axis=1, tiled=True),
    )

    def key_tile(tile_index):
        tile_start = tile_index * key_block
        key_pos = tile_start + jnp.arange(key_block, dtype=jnp.int32)
        key_part = lax.dynamic_slice_in_dim(keys_all, tile_start, key_block, 1).reshape(
            rows_dev, key_block, kv_heads, head_dim
        )
        value_part = lax.dynamic_slice_in_dim(values_all, tile_start, key_block, 1).reshape(
            rows_dev, key_block, kv_heads, head_dim
        )
        scores = (
            jnp.einsum("rqhgd,rkhd->rhgqk", queries, key_part, preferred_element_type=jnp.float32)
            * score_scale
        )
        allowed = (key_pos[None, None, :] <= slot_pos[None, :, None]) & (
            key_pos[None, None, :] < lengths[:, None, None]
        )
        return (tile_start, scores, allowed[:, None, None], key_part, value_part)

    stat_shape = (rows_dev, kv_heads, group_size, block_len)

    def stats_step(tile_index, carried):
        running_max, running_sum = carried
        tile_start, scores, allowed, key_part, value_part = key_tile(tile_index)
        masked = jnp.where(allowed, scores, NEGATIVE)
        new_max = jnp.maximum(running_max, jnp.max(masked, axis=-1))
        terms = jnp.where(allowed, jnp.exp(masked - new_max[..., None]), 0.0)
        return (new_max, running_sum * jnp.exp(running_max - new_max) + jnp.sum(terms, axis=-1))

    running_max, running_sum = lax.fori_loop(
        0,
        tiles_used,
        stats_step,
        (jnp.full(stat_shape, NEGATIVE, jnp.float32), jnp.zeros(stat_shape, jnp.float32)),
    )
    log_total = running_max + jnp.log(running_sum)
    out_shape = (rows_dev, block_len, kv_heads, group_size, head_dim)

    def value_step(tile_index, carried):
        rounded_out, exact_out = carried
        tile_start, scores, allowed, key_part, value_part = key_tile(tile_index)
        tile_probs = jnp.where(allowed, jnp.exp(scores - log_total[..., None]), 0.0)
        rounded_out = rounded_out + jnp.einsum(
            "rhgqk,rkhd->rqhgd",
            tile_probs.astype(jnp.bfloat16),
            value_part,
            preferred_element_type=jnp.float32,
        )
        exact_out = exact_out + jnp.einsum(
            "rhgqk,rkhd->rqhgd", tile_probs, value_part.astype(jnp.float32)
        )
        return (rounded_out, exact_out)

    rounded_out, exact_out = lax.fori_loop(
        0,
        tiles_used,
        value_step,
        (jnp.zeros(out_shape, jnp.float32), jnp.zeros(out_shape, jnp.float32)),
    )
    attended = rounded_out.astype(jnp.bfloat16).reshape(count_tok, q_heads * head_dim)
    attn_total = lax.psum(linear(attended, w_output), "tp")
    resid = inputs + attn_total.reshape(rows_dev, block_len, model_width)
    normed_two, back_two = jax.vjp(rms_scale, resid, gain_two_f)
    normed_second = normed_two.astype(jnp.bfloat16).reshape(count_tok, model_width)
    gate_act = linear(normed_second, w_gate)
    up_act = linear(normed_second, w_upper)
    hidden_full, back_glu = jax.vjp(swiglu, gate_act, up_act)
    hidden = hidden_full.astype(jnp.bfloat16)
    ffn_total = lax.psum(linear(hidden, w_down), "tp")
    result = resid + ffn_total.reshape(rows_dev, block_len, model_width)
    error_value = result - teacher.astype(jnp.float32)
    valid_col = valid[..., None]
    total_square, total_count = lax.psum(
        (jnp.sum(valid_col * error_value * error_value), jnp.sum(valid)), ("fsdp", "ctx")
    )
    teacher_loss = total_square / (total_count * model_width)
    grad_result = valid_col * error_value * (slots / total_count)
    grad_low = grad_result.astype(jnp.bfloat16).reshape(count_tok, model_width)
    grad_down = linear_left(hidden, grad_low)
    grad_hidden = linear_right(grad_low, w_down)
    grad_gate_full, grad_up_full = back_glu(grad_hidden)
    grad_gate = grad_gate_full.astype(jnp.bfloat16)
    grad_up = grad_up_full.astype(jnp.bfloat16)
    grad_wgate = linear_left(normed_second, grad_gate)
    grad_wup = linear_left(normed_second, grad_up)
    normed_two_part = linear_right(grad_gate, w_gate) + linear_right(grad_up, w_upper)
    grad_normed_two = lax.psum(normed_two_part, "tp")
    grad_resid_norm, grad_gain_two = back_two(
        grad_normed_two.reshape(rows_dev, block_len, model_width)
    )
    grad_resid = grad_result + grad_resid_norm
    grad_attn_low = grad_resid.astype(jnp.bfloat16).reshape(count_tok, model_width)
    grad_woutput = linear_left(attended, grad_attn_low)
    grad_attended = linear_right(grad_attn_low, w_output).astype(jnp.bfloat16).reshape(out_shape)
    delta = jnp.einsum("rqhgd,rqhgd->rhgq", grad_attended.astype(jnp.float32), exact_out)
    full_shape = (rows_dev, row_len, kv_heads * head_dim)

    def grad_step(tile_index, carried):
        grad_queries, grad_keys, grad_values = carried
        tile_start, scores, allowed, key_part, value_part = key_tile(tile_index)
        tile_probs = jnp.where(allowed, jnp.exp(scores - log_total[..., None]), 0.0)
        grad_probs = jnp.einsum(
            "rqhgd,rkhd->rhgqk", grad_attended, value_part, preferred_element_type=jnp.float32
        )
        grad_scores = (tile_probs * (grad_probs - delta[..., None])).astype(jnp.bfloat16)
        grad_queries = (
            grad_queries
            + jnp.einsum(
                "rhgqk,rkhd->rqhgd", grad_scores, key_part, preferred_element_type=jnp.float32
            )
            * score_scale
        )
        key_term = (
            jnp.einsum(
                "rhgqk,rqhgd->rkhd", grad_scores, queries, preferred_element_type=jnp.float32
            )
            * score_scale
        )
        value_term = jnp.einsum(
            "rhgqk,rqhgd->rkhd",
            tile_probs.astype(jnp.bfloat16),
            grad_attended,
            preferred_element_type=jnp.float32,
        )
        grad_keys = lax.dynamic_update_slice_in_dim(
            grad_keys, key_term.reshape(rows_dev, key_block, kv_heads * head_dim), tile_start, 1
        )
        grad_values = lax.dynamic_update_slice_in_dim(
            grad_values, value_term.reshape(rows_dev, key_block, kv_heads * head_dim), tile_start, 1
        )
        return (grad_queries, grad_keys, grad_values)

    grad_queries, grad_keys, grad_values = lax.fori_loop(
        0,
        tiles_used,
        grad_step,
        (
            jnp.zeros(out_shape, jnp.float32),
            jnp.zeros(full_shape, jnp.float32),
            jnp.zeros(full_shape, jnp.float32),
        ),
    )
    key_grad, value_grad = (
        lax.psum_scatter(grad_keys, "ctx", scatter_dimension=1, tiled=True),
        lax.psum_scatter(grad_values, "ctx", scatter_dimension=1, tiled=True),
    )
    grad_query_raw, grad_gain_query = query_back(
        grad_queries.reshape(rows_dev, block_len, q_heads, head_dim)
    )
    grad_key_raw, grad_gain_key = key_back(
        key_grad.reshape(rows_dev, block_len, kv_heads, head_dim)
    )
    query_low = grad_query_raw.astype(jnp.bfloat16)
    key_low = grad_key_raw.astype(jnp.bfloat16)
    value_low = value_grad.reshape(count_tok, kv_heads * head_dim).astype(jnp.bfloat16)
    grad_wquery = linear_left(normed_low, query_low)
    grad_wkey = linear_left(normed_low, key_low)
    grad_wvalue = linear_left(normed_low, value_low)
    normed_part = (
        linear_right(query_low, w_query)
        + linear_right(key_low, w_key)
        + linear_right(value_low, w_value)
    )
    grad_normed_one, grad_gain_query, grad_gain_key = lax.psum(
        (normed_part, grad_gain_query, grad_gain_key), "tp"
    )
    grad_input_norm, grad_gain_one = back_one(
        grad_normed_one.reshape(rows_dev, block_len, model_width)
    )
    tokens_grad = grad_resid + grad_input_norm
    partials = (
        grad_gain_one,
        grad_wquery,
        grad_wkey,
        grad_wvalue,
        grad_gain_query,
        grad_gain_key,
        grad_woutput,
        grad_gain_two,
        grad_wgate,
        grad_wup,
        grad_down,
    )
    pieces = (
        lax.psum_scatter(partials[0], ("fsdp", "ctx"), scatter_dimension=0, tiled=True),
        lax.psum_scatter(partials[1], ("fsdp", "ctx"), scatter_dimension=0, tiled=True),
        lax.psum_scatter(partials[2], ("fsdp", "ctx"), scatter_dimension=0, tiled=True),
        lax.psum_scatter(partials[3], ("fsdp", "ctx"), scatter_dimension=0, tiled=True),
        lax.psum_scatter(partials[4], ("fsdp", "ctx"), scatter_dimension=0, tiled=True),
        lax.psum_scatter(partials[5], ("fsdp", "ctx"), scatter_dimension=0, tiled=True),
        lax.psum_scatter(partials[6], ("fsdp", "ctx"), scatter_dimension=1, tiled=True),
        lax.psum_scatter(partials[7], ("fsdp", "ctx"), scatter_dimension=0, tiled=True),
        lax.psum_scatter(partials[8], ("fsdp", "ctx"), scatter_dimension=0, tiled=True),
        lax.psum_scatter(partials[9], ("fsdp", "ctx"), scatter_dimension=0, tiled=True),
        lax.psum_scatter(partials[10], ("fsdp", "ctx"), scatter_dimension=1, tiled=True),
    )
    summed = (
        lax.all_gather(pieces[0], "ctx", axis=0, tiled=True),
        lax.all_gather(pieces[1], "ctx", axis=0, tiled=True),
        lax.all_gather(pieces[2], "ctx", axis=0, tiled=True),
        lax.all_gather(pieces[3], "ctx", axis=0, tiled=True),
        lax.all_gather(pieces[4], "ctx", axis=0, tiled=True),
        lax.all_gather(pieces[5], "ctx", axis=0, tiled=True),
        lax.all_gather(pieces[6], "ctx", axis=1, tiled=True),
        lax.all_gather(pieces[7], "ctx", axis=0, tiled=True),
        lax.all_gather(pieces[8], "ctx", axis=0, tiled=True),
        lax.all_gather(pieces[9], "ctx", axis=0, tiled=True),
        lax.all_gather(pieces[10], "ctx", axis=1, tiled=True),
    )
    return (
        result.astype(jnp.bfloat16),
        teacher_loss,
        tokens_grad,
        summed[0],
        summed[1],
        summed[2],
        summed[3],
        summed[4],
        summed[5],
        summed[6],
        summed[7],
        summed[8],
        summed[9],
        summed[10],
    )


BF16 = jnp.bfloat16
F32 = jnp.float32
LOG2E = math.log2(math.e)
X_SWAP = [(0, 2), (2, 0), (1, 3), (3, 1)]
CORE_SWAP = [(0, 1), (1, 0), (2, 3), (3, 2)]
Y_SWAP = [(0, 1), (1, 0)]
Z_UP = [(0, 1), (1, 2), (2, 3), (3, 0)]
Z_DOWN = [(0, 3), (1, 0), (2, 1), (3, 2)]
Z_NEAR = [(0, 1), (1, 0), (2, 3), (3, 2)]
Z_FAR = [(0, 2), (2, 0), (1, 3), (3, 1)]
MASKS = (0, 2, 1, 3)
ANY = pl.BlockSpec(memory_space=pl.ANY)
SMEM = pl.BlockSpec(memory_space=pltpu.SMEM)


def fits(mesh):
    return dict(mesh.shape) == {"fsdp": 4, "ctx": 2, "tp": 4}


def dot(left, right, left_dim, right_dim):
    return lax.dot_general(
        left, right, (((left_dim,), (right_dim,)), ((), ())), preferred_element_type=F32
    )


def sigmoid(v):
    return 0.5 * jnp.tanh(0.5 * v) + 0.5


def whole(shape):
    zeros = (0,) * len(shape)
    return pl.BlockSpec(shape, lambda *_: zeros, pipeline_mode=pl.Buffered(1))


def settings(dims, mib):
    return pltpu.CompilerParams(
        dimension_semantics=("arbitrary",) * dims, vmem_limit_bytes=mib << 20
    )


def shape_of(shape, dtype):
    return jax.ShapeDtypeStruct(shape, dtype)


def cost(large):
    size = 1 << 42 if large else 1 << 10
    return pl.CostEstimate(flops=size, bytes_accessed=size >> 12, transcendentals=0)


def pack_kernel(info, o_in, g_in, u_in, d_in, *refs):
    out_ref, ffn_ref, *chunk_refs, others_ref, o_ref, g_ref, u_ref, d_ref, sems = refs
    ctx = info[2]
    pairs = ((o_in, o_ref), (g_in, g_ref), (u_in, u_ref), (d_in, d_ref))
    copies = [pltpu.make_async_copy(a, b, sems.at[i]) for i, (a, b) in enumerate(pairs)]
    for copy in copies:
        copy.start()
    for copy in copies:
        copy.wait()
    out_ref[...] = o_ref[...].astype(F32).T.astype(BF16)
    third = g_ref.shape[1] // 3
    for j in range(3):
        at = pl.multiple_of(jnp.where(ctx == 0, j, 2 - j) * third, third)
        parts = [
            g_ref[:, pl.ds(at, third)],
            u_ref[:, pl.ds(at, third)],
            d_ref[pl.ds(at, third), :].astype(F32).T.astype(BF16),
        ]
        for i, part in enumerate(parts):
            chunk_refs[j][:, i * third : (i + 1) * third] = part
            if j:
                others_ref[:, (3 * j - 3 + i) * third : (3 * j - 2 + i) * third] = part
            ffn_ref[:, (3 * j + i) * third : (3 * j + i + 1) * third] = part


def pack(info, o, g, u, d):
    rows, units = g.shape
    feats = o.shape[0]
    widths = (feats, 3 * units, units, units, units, 2 * units)
    return pl.pallas_call(
        pack_kernel,
        in_specs=[SMEM] + [ANY] * 4,
        out_specs=[pl.BlockSpec(memory_space=pltpu.VMEM)] * 6,
        out_shape=[shape_of((rows, n), BF16) for n in widths],
        scratch_shapes=[pltpu.VMEM(a.shape, BF16) for a in (o, g, u, d)]
        + [pltpu.SemaphoreType.DMA((4,))],
        compiler_params=pltpu.CompilerParams(vmem_limit_bytes=24 << 20),
        cost_estimate=cost(False),
        name="pack",
    )(info, o, g, u, d)


def join_kernel(q_ref, k_ref, v_ref, out_ref):
    at = 0
    for ref in (q_ref, k_ref, v_ref):
        out_ref[:, at : at + ref.shape[1]] = ref[...]
        at += ref.shape[1]


def join(q, k, v):
    return pl.pallas_call(
        join_kernel,
        out_shape=shape_of((q.shape[0], q.shape[1] + k.shape[1] + v.shape[1]), BF16),
        compiler_params=pltpu.CompilerParams(vmem_limit_bytes=8 << 20),
        cost_estimate=cost(False),
        name="join",
    )(q, k, v)


def norm_one_kernel(info, tok_ref, gain_ref, x_ref, nt_ref, x32):
    quarter = x_ref.shape[1] // 4
    for p, mask in enumerate(MASKS):
        at = pl.multiple_of(jnp.bitwise_xor(info[1], mask) * quarter, quarter)
        part = tok_ref[0, :, pl.ds(at, quarter)]
        x_ref[:, p * quarter : (p + 1) * quarter] = part
        x32[:, p * quarter : (p + 1) * quarter] = part.astype(F32)
    x = x32[...]
    rho = lax.rsqrt(jnp.mean(x * x, axis=-1, keepdims=True) + EPS)
    nt_ref[...] = (x * rho * gain_ref[...]).T.astype(BF16)


def norm_one(info, tokens, gain, tile):
    _, tok, width = tokens.shape
    return pl.pallas_call(
        norm_one_kernel,
        grid_spec=pltpu.PrefetchScalarGridSpec(
            num_scalar_prefetch=1,
            grid=(tok // tile,),
            in_specs=[
                pl.BlockSpec((1, tile, width), lambda i, info: (info[0], i, 0)),
                pl.BlockSpec((1, width), lambda i, info: (0, 0)),
            ],
            out_specs=[
                pl.BlockSpec((tile, width), lambda i, info: (i, 0)),
                pl.BlockSpec((width, tile), lambda i, info: (0, i)),
            ],
            scratch_shapes=[pltpu.VMEM((tile, width), F32)],
        ),
        out_shape=[shape_of((tok, width), BF16), shape_of((width, tok), BF16)],
        compiler_params=settings(1, 24),
        cost_estimate=cost(False),
        name="norm_one",
    )(info, tokens, gain)


def proj_kernel(heads, block, plan, count, info, *refs):
    nt_ref, cos_ref, sin_ref, qg_ref, kg_ref, rot_ref, raw_ref, w_ref, sem = refs[count:]
    rows = w_ref.shape[0] // 4

    @pl.when(pl.program_id(0) == 0)
    def _():
        for k in range(4):

            @pl.when(block(info) == k)
            def _():
                for p, (piece, row) in enumerate(plan[k]):
                    src = refs[piece].at[pl.ds(row, rows)]
                    pltpu.make_async_copy(src, w_ref.at[pl.ds(p * rows, rows)], sem).start()

        pltpu.make_async_copy(w_ref, w_ref, sem).wait()

    hd = qg_ref.shape[0]
    half = hd // 2
    raw = dot(w_ref[...], nt_ref[...], 0, 0)
    cos_part, sin_part = cos_ref[...], sin_ref[...]
    heads_q, heads_k = heads
    raw_ref[...] = raw.astype(BF16)
    for h in range(heads_q + heads_k):
        v = raw[h * hd : (h + 1) * hd]
        rho = lax.rsqrt(jnp.mean(v * v, axis=0, keepdims=True) + EPS)
        v = v * rho * (qg_ref[...] if h < heads_q else kg_ref[...])
        a, b = v[:half], v[half:]
        rot_ref[h * hd : h * hd + half, :] = (a * cos_part - b * sin_part).astype(BF16)
        rot_ref[h * hd + half : (h + 1) * hd, :] = (b * cos_part + a * sin_part).astype(BF16)
    at = (heads_q + heads_k) * hd
    rot_ref[at:, :] = raw[at:].astype(BF16)


def project(info, weights, normed_t, cos_part, sin_part, gain_q, gain_k, heads, block):
    plan, pieces = weights
    width, tok = normed_t.shape
    cols = pieces[0].shape[1]
    tile = min(512, tok)
    const = lambda a: pl.BlockSpec(a.shape, lambda i, info: (0, 0))
    tab = lambda a: pl.BlockSpec((a.shape[0], tile), lambda i, info: (0, i))
    return pl.pallas_call(
        functools.partial(proj_kernel, heads, block, plan, len(pieces)),
        grid_spec=pltpu.PrefetchScalarGridSpec(
            num_scalar_prefetch=1,
            grid=(tok // tile,),
            in_specs=[ANY] * len(pieces)
            + [tab(normed_t), tab(cos_part), tab(sin_part), const(gain_q), const(gain_k)],
            out_specs=[pl.BlockSpec((cols, tile), lambda i, info: (0, i))] * 2,
            scratch_shapes=[pltpu.VMEM((width, cols), BF16), pltpu.SemaphoreType.DMA],
        ),
        out_shape=[shape_of((cols, tok), BF16), shape_of((cols, tok), BF16)],
        compiler_params=settings(1, 24),
        cost_estimate=cost(False),
        name="project",
    )(info, *pieces, normed_t, cos_part, sin_part, gain_q, gain_k)


def head_back_kernel(
    heads, info, dm_ref, dt_ref, rm_ref, rt_ref, cos_ref, sin_ref, qg_ref, kg_ref, out_ref, gg_ref
):
    step, part = pl.program_id(0), pl.program_id(1)
    hd = qg_ref.shape[0]
    half = hd // 2
    heads_q, heads_k = heads
    cos_part, sin_part = cos_ref[...], sin_ref[...]
    tile = cos_part.shape[1]

    @pl.when((step == 0) & (part == 0))
    def _():
        gg_ref[...] = jnp.zeros_like(gg_ref)

    def work(d_ref, r_ref):
        gain_q = jnp.zeros((hd, 1), F32)
        gain_k = jnp.zeros((hd, 1), F32)
        done = []
        for h in range(heads_q + heads_k):
            is_q = h < heads_q
            g = d_ref[h * hd : (h + 1) * hd, :].astype(F32)
            raw = r_ref[h * hd : (h + 1) * hd, :].astype(F32)
            a, b = g[:half], g[half:]
            turned = jnp.concatenate(
                [a * cos_part + b * sin_part, b * cos_part - a * sin_part], axis=0
            )
            rho = lax.rsqrt(jnp.mean(raw * raw, axis=0, keepdims=True) + EPS)
            unit = raw * rho
            prod = turned * unit
            scaled = turned * (qg_ref[...] if is_q else kg_ref[...])
            mean = jnp.mean(scaled * unit, axis=0, keepdims=True)
            done.append(rho * (scaled - unit * mean))
            total = jnp.sum(prod, axis=1, keepdims=True)
            if is_q:
                gain_q = gain_q + total
            else:
                gain_k = gain_k + total
        done.append(d_ref[(heads_q + heads_k) * hd :, :].astype(F32))
        out_ref[0] = jnp.concatenate(done, axis=0).T.astype(BF16)
        lane = lax.broadcasted_iota(jnp.int32, gg_ref.shape, 1)
        gg_ref[...] += jnp.where(lane == 0, gain_q, jnp.where(lane == 1, gain_k, 0.0))

    @pl.when(step == 0)
    def _():
        work(dm_ref, rm_ref)

    @pl.when(step == 1)
    def _():
        work(dt_ref, rt_ref)


def head_back(info, grad_mine, grad_theirs, raw_mine, raw_theirs, cos_part, sin_part, gq, gk, heads):
    cols, tok = grad_mine.shape
    tile = min(512, tok)
    mine = pl.BlockSpec((cols, tile), lambda s, i, info: (0, jnp.where(s == 0, i, tok // tile - 1)))
    theirs = pl.BlockSpec((cols, tile), lambda s, i, info: (0, jnp.where(s == 0, 0, i)))
    tab = lambda a: pl.BlockSpec((a.shape[0], tile), lambda s, i, info: (0, i))
    const = lambda a: pl.BlockSpec(a.shape, lambda s, i, info: (0, 0))
    return pl.pallas_call(
        functools.partial(head_back_kernel, heads),
        grid_spec=pltpu.PrefetchScalarGridSpec(
            num_scalar_prefetch=1,
            grid=(2, tok // tile),
            in_specs=[
                mine,
                theirs,
                mine,
                theirs,
                tab(cos_part),
                tab(sin_part),
                const(gq),
                const(gk),
            ],
            out_specs=[
                pl.BlockSpec(
                    (1, tile, cols), lambda s, i, info: (jnp.bitwise_xor(info[2], s), i, 0)
                ),
                pl.BlockSpec((gq.shape[0], 128), lambda s, i, info: (0, 0)),
            ],
        ),
        out_shape=[shape_of((2, tok, cols), BF16), shape_of((gq.shape[0], 128), F32)],
        compiler_params=settings(2, 60),
        cost_estimate=cost(False),
        name="head_back",
    )(info, grad_mine, grad_theirs, raw_mine, raw_theirs, cos_part, sin_part, gq, gk)


def load_rows(info, mine_ref, got_ref, rows, sems):
    tok = mine_ref.shape[1]
    ctx = info[2]
    here = pl.multiple_of(ctx * tok, tok)
    there = pl.multiple_of((1 - ctx) * tok, tok)
    one = pltpu.make_async_copy(mine_ref, rows.at[:, pl.ds(here, tok)], sems.at[0])
    two = pltpu.make_async_copy(got_ref, rows.at[:, pl.ds(there, tok)], sems.at[1])
    one.start()
    two.start()
    one.wait()
    two.wait()


def keys_with_bias(keys, length):
    hd, slots = keys.shape
    pos = lax.broadcasted_iota(jnp.int32, (hd, slots), 1)
    row = lax.broadcasted_iota(jnp.int32, (hd, slots), 0)
    bias = jnp.where((row == 0) & (pos >= length), NEGATIVE, 0.0)
    return jnp.concatenate([keys.astype(F32), bias], axis=0).T.astype(BF16)


def query_with_one(pair):
    one_row = jnp.where(lax.broadcasted_iota(jnp.int32, pair.shape, 0) == 0, 1.0, 0.0)
    return jnp.concatenate([pair, one_row.astype(BF16)], axis=0)


def by_halves(left, right):
    half = left.shape[1] // 2
    return jnp.concatenate(
        [left[:, :half], right[:, :half], left[:, half:], right[:, half:]], axis=1
    )


def by_heads(both):
    quarter = both.shape[1] // 4
    part = lambda i: both[:, i * quarter : (i + 1) * quarter]
    return (
        jnp.concatenate([part(0), part(2)], axis=1),
        jnp.concatenate([part(1), part(3)], axis=1),
    )


def causal(scores):
    half = scores.shape[0]
    key_pos = lax.broadcasted_iota(jnp.int32, (half, half), 0)
    query_pos = lax.broadcasted_iota(jnp.int32, (half, half), 1)
    allowed = key_pos <= query_pos
    return jnp.where(jnp.concatenate([allowed, allowed], axis=1), scores, NEGATIVE)


def attn_fwd_kernel(
    width, hd, info, mine_ref, got_ref, keep_ref, send_ref, lse_ref, rows, key_rows, sems
):
    head, block = pl.program_id(0), pl.program_id(1)
    heads_k = pl.num_programs(0)
    scale = hd**-0.5 * LOG2E
    length = info[3]
    key_at = pl.multiple_of(heads_k * 2 * hd + head * hd, hd)
    value_at = pl.multiple_of(heads_k * 3 * hd + head * hd, hd)
    query_at = pl.multiple_of(head * 2 * hd, 2 * hd)

    @pl.when((head == 0) & (block == 0))
    def _():
        load_rows(info, mine_ref, got_ref, rows, sems)

    @pl.when(block == 0)
    def _():
        key_rows[...] = keys_with_bias(rows[pl.ds(key_at, hd), :], length)

    start = pl.multiple_of(block * width, width)
    both = rows[pl.ds(query_at, 2 * hd), pl.ds(start, width)]
    query = query_with_one(by_halves(both[:hd], both[hd:]))
    half = width // 2

    def terms(at, keys, query, mask):
        scores = dot(key_rows[pl.ds(at, keys), :], query, 1, 0)
        if mask:
            part = causal(scores[:, :width])
            wide = scores.shape[1] > width
            scores = jnp.concatenate([part, scores[:, width:]], axis=1) if wide else part
        probs = jnp.exp2(scores * scale)
        total = jnp.sum(probs, axis=0, keepdims=True)
        return dot(rows[pl.ds(value_at, hd), pl.ds(at, keys)], probs.astype(BF16), 1, 0), total

    def tile(at, carried):
        more, sums = terms(at, width, query, False)
        return carried[0] + more, carried[1] + sums

    carried = (jnp.zeros((hd, 2 * width), F32), jnp.zeros((1, 2 * width), F32))
    full = jnp.minimum(block, lax.div(length + width - 1, width))
    carried = lax.fori_loop(
        0, full, lambda j, c: tile(pl.multiple_of(j * width, width), c), carried
    )
    more, sums = terms(start, half, query, True)
    out, total = carried[0] + more, carried[1] + sums
    later = pl.multiple_of(start + half, half)
    more, sums = terms(later, half, query[:, width:], True)
    out = jnp.concatenate([out[:, :width], out[:, width:] + more], axis=1)
    total = jnp.concatenate([total[:, :width], total[:, width:] + sums], axis=1)
    out = out * (1.0 / total)
    out = jnp.concatenate(by_heads(out), axis=0).T.astype(BF16)
    here = block // 2 == info[2]

    @pl.when(here)
    def _():
        keep_ref[...] = out

    @pl.when(jnp.logical_not(here))
    def _():
        send_ref[...] = out

    log_first, log_second = by_heads(jnp.log2(total))
    lse_ref[0, 0:1, :] = log_first
    lse_ref[0, 1:2, :] = log_second


def keep_block(i, info):
    return jnp.clip(i - 2 * info[2], 0, 1)


def send_block(i, info):
    return jnp.clip(i - 2 * (1 - info[2]), 0, 1)


def attn_fwd(info, mine, got, hd):
    cols, tok = mine.shape
    heads_k = cols // (4 * hd)
    width = tok // 2
    return pl.pallas_call(
        functools.partial(attn_fwd_kernel, width, hd),
        grid_spec=pltpu.PrefetchScalarGridSpec(
            num_scalar_prefetch=1,
            grid=(heads_k, 4),
            in_specs=[ANY, ANY],
            out_specs=[
                pl.BlockSpec((width, 2 * hd), lambda h, i, info: (keep_block(i, info), h)),
                pl.BlockSpec((width, 2 * hd), lambda h, i, info: (send_block(i, info), h)),
                pl.BlockSpec((1, 2, width), lambda h, i, info: (h, 0, i)),
            ],
            scratch_shapes=[
                pltpu.VMEM((cols, 2 * tok), BF16),
                pltpu.VMEM((2 * tok, 2 * hd), BF16),
                pltpu.SemaphoreType.DMA((2,)),
            ],
        ),
        out_shape=[
            shape_of((tok, heads_k * 2 * hd), BF16),
            shape_of((tok, heads_k * 2 * hd), BF16),
            shape_of((heads_k, 2, 2 * tok), F32),
        ],
        compiler_params=settings(2, 60),
        cost_estimate=cost(True),
        name="attn_fwd",
    )(info, mine, got)


def attn_bwd_kernel(
    width,
    hd,
    info,
    mine_ref,
    got_ref,
    ok_ref,
    os_ref,
    gk_ref,
    gs_ref,
    lse_ref,
    keep_ref,
    send_ref,
    rows,
    key_rows,
    value_rows,
    key_sum,
    value_sum,
    sems,
):
    head, block = pl.program_id(0), pl.program_id(1)
    heads_k = pl.num_programs(0)
    scale = hd**-0.5
    length = info[3]
    ctx = info[2]
    tok = keep_ref.shape[1]
    key_at = pl.multiple_of(heads_k * 2 * hd + head * hd, hd)
    value_at = pl.multiple_of(heads_k * 3 * hd + head * hd, hd)
    query_at = pl.multiple_of(head * 2 * hd, 2 * hd)

    @pl.when((head == 0) & (block == 0))
    def _():
        load_rows(info, mine_ref, got_ref, rows, sems)

    @pl.when(block == 0)
    def _():
        key_rows[...] = keys_with_bias(rows[pl.ds(key_at, hd), :], length)
        value_rows[...] = rows[pl.ds(value_at, hd), :].astype(F32).T.astype(BF16)
        key_sum[...] = jnp.zeros_like(key_sum)
        value_sum[...] = jnp.zeros_like(value_sum)

    start = pl.multiple_of(block * width, width)
    here = block // 2 == ctx

    def store_query(value):
        at = pl.ds(pl.multiple_of((block % 2) * width, width), width)

        @pl.when(here)
        def _():
            keep_ref[pl.ds(query_at, 2 * hd), at] = value

        @pl.when(jnp.logical_not(here))
        def _():
            send_ref[pl.ds(query_at, 2 * hd), at] = value

    @pl.when(block * width < length)
    def _():
        both = rows[pl.ds(query_at, 2 * hd), pl.ds(start, width)]
        pair = by_halves(both[:hd], both[hd:])
        query = query_with_one(pair)
        query_rows = pair.astype(F32).T.astype(BF16)
        grad_wide = jnp.where(here, gk_ref[...].astype(F32), gs_ref[...].astype(F32))
        out_wide = jnp.where(here, ok_ref[...].astype(F32), os_ref[...].astype(F32))
        grad_t = grad_wide.T
        prod = (grad_wide * out_wide).T
        grad = by_halves(grad_t[:hd], grad_t[hd:]).astype(BF16)
        half = width // 2
        grad_rows = jnp.concatenate(
            [
                grad_wide[:half, :hd],
                grad_wide[:half, hd:],
                grad_wide[half:, :hd],
                grad_wide[half:, hd:],
            ],
            axis=0,
        ).astype(BF16)
        delta = by_halves(
            jnp.sum(prod[:hd], axis=0, keepdims=True), jnp.sum(prod[hd:], axis=0, keepdims=True)
        )
        lse = by_halves(lse_ref[0, 0:1, :], lse_ref[0, 1:2, :])

        def terms(at, keys, first, mask):
            scores = dot(key_rows[pl.ds(at, keys), :], query[:, first:], 1, 0)
            if mask:
                part = causal(scores[:, :width])
                wide = scores.shape[1] > width
                scores = jnp.concatenate([part, scores[:, width:]], axis=1) if wide else part
            probs = jnp.exp2(scores * (scale * LOG2E) - lse[:, first:])
            grad_probs = dot(value_rows[pl.ds(at, keys), :], grad[:, first:], 1, 0)
            grad_scores = (probs * (grad_probs - delta[:, first:])).astype(BF16)
            value_sum[pl.ds(at, keys), :] += dot(probs.astype(BF16), grad_rows[first:], 1, 0)
            key_sum[pl.ds(at, keys), :] += dot(grad_scores, query_rows[first:], 1, 0)
            return dot(rows[pl.ds(key_at, hd), pl.ds(at, keys)], grad_scores, 1, 0)

        query_sum = lax.fori_loop(
            0,
            block,
            lambda j, s: s + terms(pl.multiple_of(j * width, width), width, 0, False),
            jnp.zeros((hd, 2 * width), F32),
        )
        query_sum = query_sum + terms(start, half, 0, True)
        later = terms(pl.multiple_of(start + half, half), half, width, True)
        query_sum = jnp.concatenate([query_sum[:, :width], query_sum[:, width:] + later], axis=1)
        store_query(jnp.concatenate(by_heads(query_sum * scale), axis=0).astype(BF16))

    @pl.when(block * width >= length)
    def _():
        store_query(jnp.zeros((2 * hd, width), BF16))

    @pl.when(block == 3)
    def _():
        for at, total in ((key_at, key_sum[...] * scale), (value_at, value_sum[...])):
            total = total.T.astype(BF16)
            left, right = total[:, :tok], total[:, tok:]

            @pl.when(ctx == 0)
            def _():
                keep_ref[pl.ds(at, hd), :] = left
                send_ref[pl.ds(at, hd), :] = right

            @pl.when(ctx == 1)
            def _():
                keep_ref[pl.ds(at, hd), :] = right
                send_ref[pl.ds(at, hd), :] = left


def attn_bwd(info, mine, got, out_keep, out_send, grad_keep, grad_send, lse, hd):
    cols, tok = mine.shape
    heads_k = cols // (4 * hd)
    width = tok // 2
    keep = pl.BlockSpec((width, 2 * hd), lambda h, i, info: (keep_block(i, info), h))
    send = pl.BlockSpec((width, 2 * hd), lambda h, i, info: (send_block(i, info), h))
    full = pl.BlockSpec((cols, tok), lambda h, i, info: (0, 0))
    return pl.pallas_call(
        functools.partial(attn_bwd_kernel, width, hd),
        grid_spec=pltpu.PrefetchScalarGridSpec(
            num_scalar_prefetch=1,
            grid=(heads_k, 4),
            in_specs=[
                ANY,
                ANY,
                keep,
                send,
                keep,
                send,
                pl.BlockSpec((1, 2, width), lambda h, i, info: (h, 0, i)),
            ],
            out_specs=[full, full],
            scratch_shapes=[
                pltpu.VMEM((cols, 2 * tok), BF16),
                pltpu.VMEM((2 * tok, 2 * hd), BF16),
                pltpu.VMEM((2 * tok, hd), BF16),
                pltpu.VMEM((2 * tok, hd), F32),
                pltpu.VMEM((2 * tok, hd), F32),
                pltpu.SemaphoreType.DMA((2,)),
            ],
        ),
        out_shape=[shape_of((cols, tok), BF16), shape_of((cols, tok), BF16)],
        compiler_params=settings(2, 60),
        cost_estimate=cost(True),
        name="attn_bwd",
    )(info, mine, got, out_keep, out_send, grad_keep, grad_send, lse)


def load_blocks(plan, pieces, target, sem):
    rows = target.shape[1] // 4

    @pl.when(pl.program_id(0) == 0)
    def _():
        for k, places in enumerate(plan):
            for p, (piece, row) in enumerate(places):
                src = pieces[piece].at[pl.ds(row, rows)]
                pltpu.make_async_copy(src, target.at[k, pl.ds(p * rows, rows)], sem).start()
        pltpu.make_async_copy(target, target, sem).wait()


def out_proj_kernel(plan, count, info, *refs):
    x_ref, a0, a1, b0, b1, gain_ref, r_ref, n_ref, nt_ref, att_ref, w_ref, sem = refs[count:]
    load_blocks(plan, refs, w_ref, sem)
    ctx = info[2]
    total = x_ref[...].astype(F32)
    for j, ref, side in ((0, a0, ctx), (1, a1, ctx), (0, b0, 1 - ctx), (1, b1, 1 - ctx)):
        block = 2 * side + j
        part = ref[...]
        att_ref[block] = part
        total = total + dot(part, w_ref[block], 1, 1)
    rho = lax.rsqrt(jnp.mean(total * total, axis=-1, keepdims=True) + EPS)
    normed = total * rho * gain_ref[...]
    r_ref[...] = total
    n_ref[...] = normed.astype(BF16)
    nt_ref[...] = normed.T.astype(BF16)


def out_proj(info, x, mine, theirs, weights, gain, tile):
    plan, pieces = weights
    tok, width = x.shape
    feats = pieces[0].shape[1]
    rows_of = lambda n: pl.BlockSpec((tile, n), lambda i, info: (i, 0))
    return pl.pallas_call(
        functools.partial(out_proj_kernel, plan, len(pieces)),
        grid_spec=pltpu.PrefetchScalarGridSpec(
            num_scalar_prefetch=1,
            grid=(tok // tile,),
            in_specs=[ANY] * len(pieces)
            + [rows_of(width)]
            + [rows_of(feats)] * 4
            + [pl.BlockSpec((1, width), lambda i, info: (0, 0))],
            out_specs=[
                rows_of(width),
                rows_of(width),
                pl.BlockSpec((width, tile), lambda i, info: (0, i)),
                pl.BlockSpec((4, tile, feats), lambda i, info: (0, i, 0)),
            ],
            scratch_shapes=[pltpu.VMEM((4, width, feats), BF16), pltpu.SemaphoreType.DMA],
        ),
        out_shape=[
            shape_of((tok, width), F32),
            shape_of((tok, width), BF16),
            shape_of((width, tok), BF16),
            shape_of((4, tok, feats), BF16),
        ],
        compiler_params=settings(1, 60),
        cost_estimate=cost(True),
        name="out_proj",
    )(info, *pieces, x, *mine, *theirs, gain)


def norm_two_back_kernel(plan, count, info, *refs):
    g_ref, r_ref, gr_ref, gain_ref, gres_ref, gat_ref, a0, a1, b0, b1, gg_ref, w_ref, sem = refs[count:]
    load_blocks(plan, refs, w_ref, sem)
    ctx = info[2]
    grad, resid = g_ref[...], r_ref[...]
    rho = lax.rsqrt(jnp.mean(resid * resid, axis=-1, keepdims=True) + EPS)
    unit = resid * rho
    scaled = grad * gain_ref[...]
    back = rho * (scaled - unit * jnp.mean(scaled * unit, axis=-1, keepdims=True))
    total = gr_ref[...] + back
    gres_ref[...] = total
    low = total.astype(BF16)
    gat_ref[...] = total.T.astype(BF16)

    @pl.when(pl.program_id(0) == 0)
    def _():
        gg_ref[...] = jnp.zeros_like(gg_ref)

    gg_ref[...] += jnp.sum(grad * unit, axis=0, keepdims=True)
    for j, ref, side in ((0, a0, ctx), (1, a1, ctx), (0, b0, 1 - ctx), (1, b1, 1 - ctx)):
        ref[...] = dot(low, w_ref[2 * side + j], 1, 0).astype(BF16)


def norm_two_back(info, grad, resid, grad_result, gain, weights, tile):
    plan, pieces = weights
    tok, width = grad.shape
    feats = pieces[0].shape[1]
    rows_of = lambda n: pl.BlockSpec((tile, n), lambda i, info: (i, 0))
    row = pl.BlockSpec((1, width), lambda i, info: (0, 0))
    return pl.pallas_call(
        functools.partial(norm_two_back_kernel, plan, len(pieces)),
        grid_spec=pltpu.PrefetchScalarGridSpec(
            num_scalar_prefetch=1,
            grid=(tok // tile,),
            in_specs=[ANY] * len(pieces) + [rows_of(width)] * 3 + [row],
            out_specs=[rows_of(width), pl.BlockSpec((width, tile), lambda i, info: (0, i))]
            + [rows_of(feats)] * 4
            + [row],
            scratch_shapes=[pltpu.VMEM((4, width, feats), BF16), pltpu.SemaphoreType.DMA],
        ),
        out_shape=[shape_of((tok, width), F32), shape_of((width, tok), BF16)]
        + [shape_of((tok, feats), BF16)] * 4
        + [shape_of((1, width), F32)],
        compiler_params=settings(1, 60),
        cost_estimate=cost(True),
        name="norm_two_back",
    )(info, *pieces, grad, resid, grad_result, gain)


def norm_one_back_kernel(plan, count, info, *refs):
    p0, p1, x_ref, gres_ref, gain_ref, out_ref, gg_ref, w_ref, sem = refs[count:]
    load_blocks(plan, refs, w_ref, sem)
    quarter = x_ref.shape[1] // 4
    grad = dot(p0[0], w_ref[0], 1, 1)
    grad = grad + dot(p1[0], w_ref[1], 1, 1)
    grad = grad + dot(p0[1], w_ref[2], 1, 1)
    grad = grad + dot(p1[1], w_ref[3], 1, 1)
    x = x_ref[...].astype(F32)
    rho = lax.rsqrt(jnp.mean(x * x, axis=-1, keepdims=True) + EPS)
    unit = x * rho
    scaled = grad * gain_ref[...]
    back = rho * (scaled - unit * jnp.mean(scaled * unit, axis=-1, keepdims=True))
    total = (gres_ref[...] + back).astype(BF16)
    for p, mask in enumerate(MASKS):
        at = pl.multiple_of(jnp.bitwise_xor(info[1], mask) * quarter, quarter)
        part = total[:, p * quarter : (p + 1) * quarter]

        out_ref[:, pl.ds(at, quarter)] = part

    @pl.when(pl.program_id(0) == 0)
    def _():
        gg_ref[...] = jnp.zeros_like(gg_ref)

    gg_ref[...] += jnp.sum(grad * unit, axis=0, keepdims=True)


def norm_one_back(info, pairs, weights, x, grad_resid, gain, tile):
    plan, pieces = weights
    tok, width = x.shape
    cols = pieces[0].shape[1]
    rows_of = lambda n: pl.BlockSpec((tile, n), lambda i, info: (i, 0))
    pair = pl.BlockSpec((2, tile, cols), lambda i, info: (0, i, 0))
    row = pl.BlockSpec((1, width), lambda i, info: (0, 0))
    return pl.pallas_call(
        functools.partial(norm_one_back_kernel, plan, len(pieces)),
        grid_spec=pltpu.PrefetchScalarGridSpec(
            num_scalar_prefetch=1,
            grid=(tok // tile,),
            in_specs=[ANY] * len(pieces) + [pair, pair, rows_of(width), rows_of(width), row],
            out_specs=[rows_of(width), row],
            scratch_shapes=[pltpu.VMEM((4, width, cols), BF16), pltpu.SemaphoreType.DMA],
        ),
        out_shape=[shape_of((tok, width), BF16), shape_of((1, width), F32)],
        compiler_params=settings(1, 60),
        cost_estimate=cost(True),
        name="norm_one_back",
    )(info, *pieces, *pairs, x, grad_resid, gain)


def weight_copies(plan, pieces, gate_up, down, gate_up_sem, down_sem):
    third = down.shape[1] // 3
    rows = down.shape[0] // 4
    wide, thin = [], []
    for p, chunks in enumerate(plan):
        block = pl.ds(p * rows, rows)
        for j, (piece, row, at) in enumerate(chunks):
            src = pieces[piece].at[pl.ds(row, rows)]
            wide.append(
                pltpu.make_async_copy(
                    src.at[:, pl.ds(at, 2 * third)],
                    gate_up.at[block, pl.ds(j * 2 * third, 2 * third)],
                    gate_up_sem,
                )
            )
            thin.append(
                pltpu.make_async_copy(
                    src.at[:, pl.ds(at + 2 * third, third)],
                    down.at[block, pl.ds(j * third, third)],
                    down_sem,
                )
            )
    return wide, thin


def split_act(act):
    third = act.shape[1] // 6
    part = lambda j: act[:, j * third : (j + 1) * third]
    return [(part(0), part(1)), (part(2), part(3)), (part(4), part(5))]


def ffn_fwd_kernel(tile, plans, last, info, scale, x_ref, in_ref, *rest):
    if last:
        teach_ref, rest = rest[0], rest[1:]
    pieces = []
    for plan in plans:
        count = 1 + max(place[0] for chunks in plan for place in chunks)
        pieces.append(rest[:count])
        rest = rest[count:]
    act_ref, hid_ref = rest[:2]
    if last:
        outa_ref, outb_ref, gres_ref, low_ref, lowt_ref, sq_ref = rest[2:8]
        gate_up, down, total, sems = rest[8:]
    else:
        sum_ref, gate_up, down, total, sems = rest[2:]
    step, part = pl.program_id(0), pl.program_id(1)
    final = len(plans) - 1
    width = x_ref.shape[1]
    quarter = width // 4
    third = down.shape[2] // 3

    def copies(s):
        return weight_copies(
            plans[s], pieces[s], gate_up.at[s], down.at[s], sems.at[s, 0], sems.at[s, 1]
        )

    @pl.when((step == 0) & (part == 0))
    def _():
        for s in range(len(plans)):
            wide, thin = copies(s)
            for copy in wide + thin:
                copy.start()

    for s in range(len(plans)):

        @pl.when((step == s) & (part == 0))
        def _():
            pltpu.make_async_copy(gate_up.at[s], gate_up.at[s], sems.at[s, 0]).wait()

    rows = pl.ds(pl.multiple_of(part * tile, tile), tile)
    act = dot(x_ref[rows, :], gate_up[step], 1, 0)
    for j, (gate, upper) in enumerate(split_act(act)):
        sig = sigmoid(gate)
        silu = gate * sig
        hid_ref[0, :, j * third : (j + 1) * third] = (silu * upper).astype(BF16)
        at = 2 * j * third
        act_ref[0, :, at : at + third] = (upper * (sig + silu - silu * sig)).astype(BF16)
        act_ref[0, :, at + third : at + 2 * third] = silu.astype(BF16)
    for s in range(len(plans)):

        @pl.when((step == s) & (part == 0))
        def _():
            pltpu.make_async_copy(down.at[s], down.at[s], sems.at[s, 1]).wait()

    grown = dot(hid_ref[0], down[step], 1, 1)

    @pl.when(step == 0)
    def _():
        total[rows, :] = in_ref[...] + grown

    @pl.when(step > 0)
    def _():
        total[rows, :] += grown

    @pl.when(step == final)
    def _():
        result = total[rows, :]
        if not last:
            sum_ref[...] = result
            return
        tok = x_ref.shape[0]
        slot = info[2] * tok + part * tile + lax.broadcasted_iota(jnp.int32, (tile, 1), 0)
        valid = jnp.where(slot < info[3], 1.0, 0.0)
        square = jnp.zeros((tile, quarter), F32)
        for p, mask in enumerate(MASKS):
            at = pl.multiple_of(jnp.bitwise_xor(info[1], mask) * quarter, quarter)
            cols = slice(p * quarter, (p + 1) * quarter)
            value = result[:, cols]
            low = value.astype(BF16)

            @pl.when(part < pl.num_programs(1) // 2)
            def _():
                outa_ref[:, pl.ds(at, quarter)] = low

            @pl.when(part >= pl.num_programs(1) // 2)
            def _():
                outb_ref[:, pl.ds(at, quarter)] = low

            error = valid * (value - teach_ref[0, :, pl.ds(at, quarter)].astype(F32))
            square = square + error * error
            grad = error * scale[0]
            gres_ref[:, cols] = grad
            low_ref[:, cols] = grad.astype(BF16)
            lowt_ref[cols, :] = grad.T.astype(BF16)

        @pl.when(part == 0)
        def _():
            sq_ref[...] = jnp.zeros_like(sq_ref)

        sq_ref[...] += jnp.sum(square, axis=0, keepdims=True)


def ffn_fwd(info, scale, x, total, teacher, weights, units, tile):
    tok, width = x.shape
    pieces = [piece for _, group in weights for piece in group]
    count = len(weights)
    last = teacher is not None
    entry = lambda s, i: jnp.where(s == 0, i, tok // tile - 1)
    leave = lambda s, i: jnp.where(s == count - 1, i, 0)
    tiles = lambda n: pl.BlockSpec((tile, n), lambda s, i, info: (leave(s, i), 0))
    slab = lambda n: pl.BlockSpec((1, tile, n), lambda s, i, info: (s, i, 0))
    in_specs = [
        SMEM,
        whole((tok, width)),
        pl.BlockSpec((tile, width), lambda s, i, info: (entry(s, i), 0)),
    ]
    out_specs = [slab(2 * units), slab(units)]
    out_shape = [shape_of((count, tok, 2 * units), BF16), shape_of((count, tok, units), BF16)]
    if last:
        in_specs.append(
            pl.BlockSpec((1, tile, width), lambda s, i, info: (info[0], leave(s, i), 0))
        )
        half = tok // tile // 2
        out_specs += [
            pl.BlockSpec(
                (tile, width), lambda s, i, info: (jnp.minimum(leave(s, i), half - 1), 0)
            ),
            pl.BlockSpec(
                (tile, width), lambda s, i, info: (jnp.maximum(leave(s, i) - half, 0), 0)
            ),
            tiles(width),
            tiles(width),
            pl.BlockSpec((width, tile), lambda s, i, info: (0, leave(s, i))),
            pl.BlockSpec((1, width // 4), lambda s, i, info: (0, 0)),
        ]
        out_shape += [
            shape_of((tok // 2, width), BF16),
            shape_of((tok // 2, width), BF16),
            shape_of((tok, width), F32),
            shape_of((tok, width), BF16),
            shape_of((width, tok), BF16),
            shape_of((1, width // 4), F32),
        ]
    else:
        out_specs.append(tiles(width))
        out_shape.append(shape_of((tok, width), F32))
    return pl.pallas_call(
        functools.partial(ffn_fwd_kernel, tile, [plan for plan, _ in weights], last),
        grid_spec=pltpu.PrefetchScalarGridSpec(
            num_scalar_prefetch=1,
            grid=(count, tok // tile),
            in_specs=in_specs + [ANY] * len(pieces),
            out_specs=out_specs,
            scratch_shapes=[
                pltpu.VMEM((count, width, 2 * units), BF16),
                pltpu.VMEM((count, width, units), BF16),
                pltpu.VMEM((tok, width), F32),
                pltpu.SemaphoreType.DMA((count, 2)),
            ],
        ),
        out_shape=out_shape,
        compiler_params=settings(2, 60),
        cost_estimate=cost(True),
        name="ffn_fwd",
    )(info, scale, x, total, *([teacher] if last else []), *pieces)


def ffn_bwd_kernel(steps, plan, first, low_ref, act_ref, hid_ref, xt_ref, lowt_ref, *rest):
    count = 1 + max(place[0] for chunks in plan for place in chunks)
    pieces, rest = rest[:count], rest[count:]
    if not first:
        in_ref, rest = rest[0], rest[1:]
    out_ref, keep_ref, send_ref, gate_up, down, dact_all, hid_all, sems = rest
    step = pl.program_id(0)
    units = down.shape[1]
    third = units // 3
    tile = low_ref.shape[0]

    @pl.when(step == 0)
    def _():
        wide, thin = weight_copies(plan, pieces, gate_up, down, sems.at[0], sems.at[1])
        for copy in thin + wide:
            copy.start()
        pltpu.make_async_copy(down, down, sems.at[1]).wait()

    @pl.when(step < steps)
    def _():
        rows = pl.ds(pl.multiple_of(step * tile, tile), tile)
        grad_hidden = dot(low_ref[...], down[...], 1, 0)
        for j, (to_gate, to_upper) in enumerate(split_act(act_ref[0])):
            grad = grad_hidden[:, j * third : (j + 1) * third]
            at = 2 * j * third
            dact_all[rows, at : at + third] = (grad * to_gate.astype(F32)).astype(BF16)
            dact_all[rows, at + third : at + 2 * third] = (grad * to_upper.astype(F32)).astype(BF16)
        hid_all[rows, :] = hid_ref[0]

        @pl.when(step == 0)
        def _():
            pltpu.make_async_copy(gate_up, gate_up, sems.at[0]).wait()

        grown = dot(dact_all[rows, :], gate_up[...], 1, 1)
        out_ref[...] = grown if first else in_ref[...] + grown

    def weight_rows(target):
        target[:, : 2 * units] = dot(xt_ref[...], dact_all[...], 1, 0).astype(BF16)
        target[:, 2 * units :] = dot(lowt_ref[...], hid_all[...], 1, 0).astype(BF16)

    @pl.when((step >= steps) & (step < steps + 2))
    def _():
        weight_rows(send_ref)

    @pl.when(step >= steps + 2)
    def _():
        weight_rows(keep_ref)


def ffn_bwd(low, saved, weights, total, xt, lowt, tile):
    plan, pieces = weights
    acts, hiddens, block = saved
    tok, width = low.shape
    units = hiddens.shape[2]
    steps = tok // tile
    quarter = width // 4
    first = total is None
    clip = lambda i: jnp.minimum(i, steps - 1)
    rows_of = lambda n: pl.BlockSpec((tile, n), lambda i: (clip(i), 0))
    slab = lambda n: pl.BlockSpec((1, tile, n), lambda i: (block, clip(i), 0))
    feature = lambda i: (jnp.where(i < steps + 2, jnp.maximum(i - steps, 0) + 2, i - steps - 2), 0)
    return pl.pallas_call(
        functools.partial(ffn_bwd_kernel, steps, plan, first),
        grid=(steps + 4,),
        in_specs=[
            rows_of(width),
            slab(2 * units),
            slab(units),
            pl.BlockSpec((quarter, tok), feature),
            pl.BlockSpec((quarter, tok), feature),
        ]
        + [ANY] * len(pieces)
        + ([] if first else [rows_of(width)]),
        out_specs=[
            rows_of(width),
            pl.BlockSpec((quarter, 3 * units), lambda i: (jnp.maximum(i - steps - 2, 0), 0)),
            pl.BlockSpec((quarter, 3 * units), lambda i: (jnp.clip(i - steps, 0, 1), 0)),
        ],
        out_shape=[
            shape_of((tok, width), F32),
            shape_of((width // 2, 3 * units), BF16),
            shape_of((width // 2, 3 * units), BF16),
        ],
        scratch_shapes=[
            pltpu.VMEM((width, 2 * units), BF16),
            pltpu.VMEM((width, units), BF16),
            pltpu.VMEM((tok, 2 * units), BF16),
            pltpu.VMEM((tok, units), BF16),
            pltpu.SemaphoreType.DMA((2,)),
        ],
        input_output_aliases={} if first else {5 + len(pieces): 0},
        compiler_params=settings(1, 60),
        cost_estimate=cost(True),
        name="ffn_bwd",
    )(low, acts, hiddens, xt, lowt, *pieces, *([] if first else [total]))


def turn_chunks(block):
    wide = block.shape[1] * 2 // 9
    thin = wide // 2
    starts = [(2 * wide, wide), (wide, wide), (0, wide)]
    starts += [(3 * wide + 2 * thin, thin), (3 * wide + thin, thin), (3 * wide, thin)]
    return jnp.concatenate([block[:, a : a + n] for a, n in starts], axis=1)


def sum_kernel(turns, *refs):
    total = None
    for ref, turn in zip(refs[:-1], turns):
        value = ref[...].astype(F32)
        value = turn_chunks(value) if turn else value
        total = value if total is None else total + value
    refs[-1][...] = total.astype(refs[-1].dtype)


def summed(terms, turns=None, dtype=BF16):
    rows, cols = terms[0].shape
    spec = pl.BlockSpec((128, cols), lambda i: (i, 0))
    return pl.pallas_call(
        functools.partial(sum_kernel, turns or [False] * len(terms)),
        grid=(rows // 128,),
        in_specs=[spec] * len(terms),
        out_specs=spec,
        out_shape=shape_of((rows, cols), dtype),
        compiler_params=settings(1, 60),
        cost_estimate=cost(False),
        name="summed",
    )(*terms)


def sums_kernel(jobs, count, info, *refs):
    arrays, refs = refs[:count], refs[count:]
    outs, (term_buf, out_buf, term_sems, out_sems) = refs[: len(jobs)], refs[len(jobs) :]
    rows = term_buf.shape[1]
    copies = []
    for terms in jobs:
        group = []
        for array, base, pick, _ in terms:
            at = base
            if pick is not None:
                at = pl.multiple_of(base + jnp.bitwise_xor(info[2], pick) * rows, rows)
            i = len(copies) + len(group)
            src = arrays[array].at[pl.ds(at, rows)]
            group.append(pltpu.make_async_copy(src, term_buf.at[i], term_sems.at[i]))
            group[-1].start()
        copies += group
    first = 0
    stores = []
    for j, terms in enumerate(jobs):
        total = None
        for i, (_, _, _, turn) in enumerate(terms):
            copies[first + i].wait()
            value = term_buf[first + i].astype(F32)
            value = turn_chunks(value) if turn else value
            total = value if total is None else total + value
        first += len(terms)
        out_buf[j] = total.astype(BF16)
        stores.append(pltpu.make_async_copy(out_buf.at[j], outs[j], out_sems.at[j]))
        stores[-1].start()
    for store in stores:
        store.wait()


def sums(info, arrays, jobs):
    cols = arrays[0].shape[1]
    rows, terms = 128, sum(len(job) for job in jobs)
    return pl.pallas_call(
        functools.partial(sums_kernel, jobs, len(arrays)),
        grid_spec=pltpu.PrefetchScalarGridSpec(
            num_scalar_prefetch=1,
            grid=(1,),
            in_specs=[ANY] * len(arrays),
            out_specs=[ANY] * len(jobs),
            scratch_shapes=[
                pltpu.VMEM((terms, rows, cols), BF16),
                pltpu.VMEM((len(jobs), rows, cols), BF16),
                pltpu.SemaphoreType.DMA((terms,)),
                pltpu.SemaphoreType.DMA((len(jobs),)),
            ],
        ),
        out_shape=[shape_of((rows, cols), BF16)] * len(jobs),
        compiler_params=settings(1, 60),
        cost_estimate=cost(False),
        name="sums",
    )(info, *arrays)


def core_jobs(keep, came):
    return [[(a, far * 256, pick, False) for a in (keep, came)] for far in (0, 1) for pick in (0, 1)]


def core_sum_kernel(info, left_ref, right_ref, *outs):
    total = (left_ref[...].astype(F32) + right_ref[...].astype(F32)).astype(BF16)
    block = pl.program_id(1)
    place = block // 2 * 2 + jnp.bitwise_xor(block % 2, info[2])
    for i, out in enumerate(outs):

        @pl.when(place == i)
        def _():
            out[...] = total


def core_sum(info, keep, came):
    groups, rows, cols = keep.shape
    spec = pl.BlockSpec((1, rows // 4, cols), lambda g, i, info: (g, i, 0))
    return pl.pallas_call(
        core_sum_kernel,
        grid_spec=pltpu.PrefetchScalarGridSpec(
            num_scalar_prefetch=1,
            grid=(groups, 4),
            in_specs=[spec] * 2,
            out_specs=[pl.BlockSpec((1, rows // 4, cols), lambda g, i, info: (g, 0, 0))] * 4,
        ),
        out_shape=[shape_of((groups, rows // 4, cols), BF16)] * 4,
        compiler_params=settings(2, 24),
        cost_estimate=cost(False),
        name="core_sum",
    )(info, keep, came)


def weight_grad_kernel(nt_ref, back0_ref, back1_ref, gt_ref, att_ref, keep_ref, send_ref):
    cols = back0_ref.shape[2]
    part, block = pl.program_id(0), pl.program_id(1)

    def rows(target, back_ref):
        target[0, :, :cols] = dot(nt_ref[...], back_ref[0], 1, 0).astype(BF16)
        target[0, :, cols:] = dot(gt_ref[...], att_ref[0], 1, 0).astype(BF16)

    for j, back_ref in enumerate((back0_ref, back1_ref)):

        @pl.when((part == 0) & (block % 2 == j))
        def _():
            rows(send_ref, back_ref)

        @pl.when((part == 1) & (block % 2 == j))
        def _():
            rows(keep_ref, back_ref)


def weight_grad(normed_t, backs, grad_t, attended):
    width, tok = normed_t.shape
    cols, feats = backs[0].shape[2], attended.shape[2]
    half = pl.BlockSpec((width // 2, tok), lambda p, k: (1 - p, 0))
    side = pl.BlockSpec((1, tok, cols), lambda p, k: (k // 2, 0, 0))
    shape = (1, width // 2, cols + feats)
    return pl.pallas_call(
        weight_grad_kernel,
        grid=(2, 4),
        in_specs=[half, side, side, half, pl.BlockSpec((1, tok, feats), lambda p, k: (k, 0, 0))],
        out_specs=[
            pl.BlockSpec(shape, lambda p, k: (jnp.where(p == 0, 0, k), 0, 0)),
            pl.BlockSpec(shape, lambda p, k: (jnp.where(p == 0, k, 3), 0, 0)),
        ],
        out_shape=[shape_of((4, width // 2, cols + feats), BF16)] * 2,
        compiler_params=settings(2, 60),
        cost_estimate=cost(True),
        name="weight_grad",
    )(normed_t, *backs, grad_t, attended)


def after(value, *others):
    return lax.optimization_barrier((value,) + others)[0]


def per_device_rows(
    tokens,
    teacher,
    lengths,
    attn_gain,
    q_weight,
    k_weight,
    v_weight,
    q_gain,
    k_gain,
    o_weight,
    ffn_gain,
    gate_weight,
    up_weight,
    down_weight,
):
    z = lax.axis_index("tp")
    ctx = lax.axis_index("ctx")
    fsdp = lax.axis_index("fsdp")
    rows_dev, tok, width = tokens.shape
    quarter = width // 4
    hd = q_gain.shape[0] * 4
    q_cols, k_cols = q_weight.shape[1], k_weight.shape[1]
    proj = q_cols + 2 * k_cols
    heads = (q_cols // hd, k_cols // hd)
    units = gate_weight.shape[1]
    slots = rows_dev * 4 * tok * 2

    def x_swap(v):
        return lax.ppermute(v, "fsdp", X_SWAP)

    def core_swap(v):
        return lax.ppermute(v, "fsdp", CORE_SWAP)

    def y_swap(v):
        return lax.ppermute(v, "ctx", Y_SWAP)

    def z_up(v):
        return lax.ppermute(v, "tp", Z_UP)

    def z_far(v):
        return lax.ppermute(v, "tp", Z_FAR)

    def z_down(v):
        return lax.ppermute(v, "tp", Z_DOWN)

    def natural(v):
        v = jnp.concatenate([v[0:1], v[2:3], v[1:2], v[3:4]], axis=0)
        v = jnp.where(fsdp % 2 == 0, v, jnp.concatenate([v[1:2], v[0:1], v[3:4], v[2:3]], axis=0))
        return jnp.where(fsdp // 2 == 0, v, jnp.concatenate([v[2:4], v[0:2]], axis=0))

    v = {}

    def sync():
        v.update(lax.optimization_barrier(dict(v)))

    length = lax.dynamic_slice_in_dim(lengths, z, 1, 0)
    info = jnp.concatenate([jnp.stack([z, fsdp, ctx]).astype(jnp.int32), length])
    w_proj = join(q_weight, k_weight, v_weight)
    proj_z = [z_up(w_proj), z_far(w_proj), z_down(w_proj)]
    proj_own = jnp.concatenate([w_proj, x_swap(w_proj)], axis=0)
    count_here = jnp.sum(lengths).astype(F32)[None]
    vector = jnp.concatenate([attn_gain, ffn_gain, q_gain, k_gain]).astype(F32)
    vector = jnp.concatenate([vector, count_here, jnp.zeros((640 - 545,), F32)])[None]
    vector = jnp.concatenate([vector, x_swap(vector)], axis=0)
    vector = jnp.concatenate([vector, core_swap(vector)], axis=0)
    w_out, w_ffn, *w_chunks = pack(info, o_weight, gate_weight, up_weight, down_weight)
    pos = (ctx * tok + jnp.arange(tok, dtype=jnp.int32)).astype(F32)
    frequency = THETA ** (-(2.0 * jnp.arange(hd // 2, dtype=F32)) / hd)
    angles = frequency[:, None] * pos[None, :]
    head_gains = natural(vector[:, 2 * quarter : 544])
    v.update(
        info=info,
        proj_own=proj_own,
        proj_z=jnp.concatenate(proj_z, axis=0),
        w_out=w_out,
        w_ffn=w_ffn,
        w_chunks=w_chunks,
        gain_one=vector[:, :quarter].reshape(1, width),
        gain_two=vector[:, quarter : 2 * quarter].reshape(1, width),
        total_count=jnp.sum(vector[:, 544]),
        gain_q=head_gains[:, : hd // 4].reshape(hd, 1),
        gain_k=head_gains[:, hd // 4 :].reshape(hd, 1),
        cos_part=jnp.cos(angles),
        sin_part=jnp.sin(angles),
    )
    sync()
    info = v["info"]

    proj_zfar = x_swap(v["proj_z"])
    out_z = [z_up(v["w_out"]), z_far(v["w_out"]), z_down(v["w_out"])]
    own_core = core_swap(v["proj_own"])
    x_in, normed_one_t = norm_one(info, tokens, v["gain_one"], 256)
    v.update(
        proj_zfar=proj_zfar, own_core=own_core, x_in=x_in, normed_one_t=normed_one_t, out_z=out_z
    )
    sync()

    plan_proj = [[(0, 0), (0, quarter), (3, 0), (3, quarter)]]
    plan_proj += [[(p, k * quarter) for p in (1, 2, 4, 5)] for k in range(3)]
    weights_proj = [v["proj_own"], v["proj_z"], v["proj_zfar"], v["own_core"]]
    weights_proj += [core_swap(v["proj_z"]), core_swap(v["proj_zfar"])]
    one = [z_up(v["w_chunks"][0]), z_up(v["w_chunks"][3])]
    ffn_far = x_swap(v["w_ffn"])
    tables = [v[name] for name in ("cos_part", "sin_part", "gain_q", "gain_k")]

    def make(block, *then):
        normed_t = after(v["normed_one_t"], *then)
        return project(info, (plan_proj, weights_proj), normed_t, *tables, heads, block)

    theirs = [make(lambda s: 2 * (1 - s[2]))]
    got = [y_swap(theirs[0][0])]
    theirs.append(make(lambda s: 2 * (1 - s[2]) + 1, theirs[0][0]))
    got.append(y_swap(theirs[1][0]))
    mine = [make(lambda s: 2 * s[2], theirs[1][0])]
    mine.append(make(lambda s: 2 * s[2] + 1, mine[0][0]))
    v.update(
        one=one,
        ffn_far=ffn_far,
        weights_proj=weights_proj,
        mine=mine,
        theirs=theirs,
        got0=got[0],
    )
    sync()

    one_far = [x_swap(v["one"][0])]
    three = [z_down(v["w_chunks"][0])]
    own_cores = [core_swap(v["w_ffn"]), core_swap(v["ffn_far"])]
    first = attn_fwd(info, v["mine"][0][0], v["got0"], hd)
    v.update(first=first, got1=got[1], one_far=one_far, three=three, own_cores=own_cores)
    sync()

    arrived = [y_swap(v["first"][1])]
    three = v["three"] + [z_down(v["w_chunks"][1])]
    out_blocks = jnp.concatenate([v["w_out"]] + v["out_z"], axis=0)
    out_far = x_swap(out_blocks)
    one_cores = [core_swap(v["one"][0]), core_swap(v["one_far"][0])]
    second = attn_fwd(info, v["mine"][1][0], v["got1"], hd)
    v.update(
        second=second,
        arrived=arrived,
        three=three,
        out_blocks=out_blocks,
        out_far=out_far,
        one_cores=one_cores,
    )
    sync()

    arrived = v["arrived"] + [y_swap(v["second"][1])]
    three = v["three"] + [z_down(v["w_chunks"][2])]
    one_far = v["one_far"] + [x_swap(v["one"][1][:, :units])]
    weights_out = [v["out_blocks"], v["out_far"]]
    weights_out += [core_swap(v["out_blocks"]), core_swap(v["out_far"])]
    v.update(arrived=arrived, three=three, one_far=one_far, weights_out=weights_out)
    sync()

    plan_out = [[(p, k * quarter) for p in range(4)] for k in range(4)]
    two = [z_up(v["one"][0])]
    three_far = [x_swap(v["three"][0])]
    one_far = v["one_far"] + [y_swap(v["one_far"][0])]
    one_cores = v["one_cores"] + [core_swap(v["one"][1]), core_swap(v["one_far"][1])]
    resid, normed_two, normed_two_t, attended = out_proj(
        info,
        v["x_in"],
        [v["first"][0], v["second"][0]],
        v["arrived"],
        (plan_out, v["weights_out"]),
        v["gain_two"],
        256,
    )
    v.update(
        two=two,
        three_far=three_far,
        one_far=one_far,
        one_cores=one_cores,
        resid=resid,
        normed_two=normed_two,
        normed_two_t=normed_two_t,
        attended=attended,
    )
    sync()

    plan0 = [[(i, 0, j * units) for j in range(3)] for i in range(4)]
    plan_mixed = [[(0, 0, 0), (1, 0, 0), (1, 0, units)], [(i, 0, 0) for i in (2, 3, 4)]]
    plan_mixed += [[(5, 0, 0), (6, 0, 0), (6, 0, units)], [(i, 0, 0) for i in (7, 8, 9)]]
    scale = (slots / v["total_count"])[None]
    weights0 = [v["w_ffn"], v["ffn_far"]] + v["own_cores"]
    c0, cf, c1, cb = v["one_cores"]
    weights1 = v["one"] + v["one_far"] + [c0, c1, cf, cb, core_swap(v["one_far"][2])]
    two = v["two"] + [z_up(v["one"][1])]
    three_far = v["three_far"] + [x_swap(v["three"][1]), y_swap(v["three_far"][0])]
    two_far = [x_swap(v["two"][0])]
    three_cores = [core_swap(v["three"][0])]
    acts_a, hiddens_a, sum_a = ffn_fwd(
        info,
        scale,
        v["normed_two"],
        v["resid"],
        None,
        [(plan0, weights0), (plan_mixed, weights1)],
        units,
        256,
    )
    v.update(
        scale=scale,
        weights0=weights0,
        weights1=weights1,
        two=two,
        three_far=three_far,
        two_far=two_far,
        three_cores=three_cores,
        acts_a=acts_a,
        hiddens_a=hiddens_a,
        sum_a=sum_a,
    )
    sync()

    plan_chunks = [[(3 * p + j, 0, 0) for j in range(3)] for p in range(4)]
    weights3 = v["three"] + v["three_far"] + v["three_cores"]
    weights3 += [core_swap(part) for part in v["three"][1:]]
    weights3 += [core_swap(part) for part in v["three_far"]]
    two_far = v["two_far"] + [x_swap(v["two"][1][:, :units]), y_swap(v["two_far"][0])]
    two_cores = [core_swap(part) for part in v["two"] + v["two_far"]]
    acts_b, hiddens_b, sum_b = ffn_fwd(
        info, v["scale"], v["normed_two"], v["sum_a"], None, [(plan_chunks, weights3)], units, 256
    )
    v.update(
        weights3=weights3,
        two_far=two_far,
        two_cores=two_cores,
        acts_b=acts_b,
        hiddens_b=hiddens_b,
        sum_b=sum_b,
    )
    sync()

    weights2 = v["two"] + v["two_far"] + v["two_cores"]
    weights2 += [core_swap(part) for part in v["two_far"][1:]]
    acts_c, hiddens_c, *results, grad_result, grad_low, grad_low_t, square = ffn_fwd(
        info, v["scale"], v["normed_two"], v["sum_b"], teacher, [(plan_mixed, weights2)], units, 256
    )
    v.update(
        weights2=weights2,
        acts_c=acts_c,
        hiddens_c=hiddens_c,
        results=results,
        grad_result=grad_result,
        grad_low=grad_low,
        grad_low_t=grad_low_t,
        square=square,
    )
    sync()

    def ffn_back(plan, weights, acts, hiddens, block, total):
        return ffn_bwd(
            v["grad_low"],
            (v[acts], v[hiddens], block),
            (plan, v[weights]),
            total,
            v["normed_two_t"],
            v["grad_low_t"],
            256,
        )

    turned = [False, False, True]
    one = [z_up(v["results"][0])]
    total, keep2, send2 = ffn_back(plan_mixed, "weights2", "acts_c", "hiddens_c", 0, None)
    v.update(one=one, total=total, keep2=keep2, send2=send2)
    sync()

    one = v["one"] + [z_up(v["results"][1])]
    came2 = core_swap(v["send2"])
    total, keep1, send1 = ffn_back(plan_mixed, "weights1", "acts_a", "hiddens_a", 1, v["total"])
    v.update(one=one, came2=came2, total=total, keep1=keep1, send1=send1)
    sync()

    out_three = [z_down(v["results"][0])]
    came1 = core_swap(v["send1"])
    sum2 = sums(info, [v["keep2"], v["came2"]], core_jobs(0, 1))
    far_t2 = x_swap(sum2[3])
    total, keep3, send3 = ffn_back(
        plan_chunks, "weights3", "acts_b", "hiddens_b", 0, after(v["total"], sum2[0])
    )
    v.update(
        out_three=out_three,
        came1=came1,
        sum2=sum2,
        far_t2=far_t2,
        total=total,
        keep3=keep3,
        send3=send3,
    )
    sync()

    out_three = v["out_three"] + [z_down(v["results"][1])]
    came3 = core_swap(v["send3"])
    far_h2 = x_swap(v["sum2"][2])
    there2, *sum1 = sums(
        info,
        [v["sum2"][1], v["far_t2"], v["keep1"], v["came1"]],
        [[(0, 0, None, False), (1, 0, None, False)]] + core_jobs(2, 3),
    )
    there2 = y_swap(there2)
    total, keep0, send0 = ffn_back(
        plan0, "weights0", "acts_a", "hiddens_a", 0, after(v["total"], sum1[0])
    )
    v.update(
        out_three=out_three,
        came3=came3,
        far_h2=far_h2,
        there2=there2,
        sum1=sum1,
        total=total,
        keep0=keep0,
        send0=send0,
    )
    sync()

    came0 = core_swap(v["send0"])
    far_t1 = x_swap(v["sum1"][3])
    plane = [(0, 0, None, False), (1, 0, None, False), (2, 0, None, True)]
    part2, *sum3 = sums(
        info,
        [v["sum2"][0], v["far_h2"], v["there2"], v["keep3"], v["came3"]],
        [plane] + core_jobs(3, 4),
    )
    down2 = z_down(part2)
    grad_resid, grad_attn_t, a0, a1, b0, b1, gain_two_sum = norm_two_back(
        info,
        after(v["total"], sum3[0]),
        v["resid"],
        v["grad_result"],
        v["gain_two"],
        (plan_out, v["weights_out"]),
        256,
    )
    grad_got = [y_swap(b0), y_swap(b1)]
    v.update(
        came0=came0,
        far_t1=far_t1,
        down2=down2,
        sum3=sum3,
        grad_resid=grad_resid,
        grad_attn_t=grad_attn_t,
        grad_mine=[a0, a1],
        gain_two_sum=gain_two_sum,
        grad_got0=grad_got[0],
    )
    sync()

    def attn_back(j, grad):
        out, got_ref = v["first" if j == 0 else "second"], v[f"got{j}"]
        return attn_bwd(
            info, v["mine"][j][0], got_ref, out[0], out[1], grad, v[f"grad_got{j}"], out[2], hd
        )

    two = [z_up(v["one"][0])]
    far_h1 = x_swap(v["sum1"][2])
    there1, *sum0 = sums(
        info,
        [v["sum1"][1], v["far_t1"], v["keep0"], v["came0"]],
        [[(0, 0, None, False), (1, 0, None, False)]] + core_jobs(2, 3),
    )
    there1 = y_swap(there1)
    far_t3 = x_swap(v["sum3"][3])
    back0 = attn_back(0, after(v["grad_mine"][0], sum0[0]))
    v.update(
        out_two=two,
        far_h1=far_h1,
        there1=there1,
        far_t3=far_t3,
        sum0=sum0,
        back0=back0,
        grad_got1=grad_got[1],
    )
    sync()

    two = v["out_two"] + [z_up(v["one"][1])]
    heads0 = y_swap(v["back0"][1])
    far_h3 = x_swap(v["sum3"][2])
    far_t0 = x_swap(v["sum0"][3])
    there3, two_down = sums(
        info,
        [v["sum3"][1], v["far_t3"], v["sum1"][0], v["far_h1"], v["there1"], v["down2"]],
        [
            [(0, 0, None, False), (1, 0, None, False)],
            [(2, 0, None, False), (3, 0, None, False), (4, 0, None, True), (5, 0, None, False)],
        ],
    )
    there3_got = y_swap(there3)
    two_down_got = z_down(two_down)
    back1 = attn_back(1, after(v["grad_mine"][1], there3, two_down))
    v.update(
        out_two=two, heads0=heads0, far_h3=far_h3, far_t0=far_t0, there3=there3_got, back1=back1
    )
    sync()

    heads1 = y_swap(v["back1"][1])
    far_h0 = x_swap(v["sum0"][2])
    part3, there0 = sums(
        info,
        [v["sum3"][0], v["far_h3"], v["there3"], v["sum0"][1], v["far_t0"]],
        [plane, [(3, 0, None, False), (4, 0, None, False)]],
    )
    up3 = z_up(part3)
    tables = [v[name] for name in ("cos_part", "sin_part", "gain_q", "gain_k")]
    head0 = head_back(
        info, v["back0"][0], v["heads0"], v["mine"][0][1], v["theirs"][0][1], *tables, heads
    )
    v.update(heads1=heads1, two_down=two_down_got, head0=head0, there0=there0)
    sync()

    there0 = y_swap(v["there0"])
    head1 = head_back(
        info, v["back1"][0], v["heads1"], v["mine"][1][1], v["theirs"][1][1], *tables, heads
    )
    tokens_low, gain_one_sum = norm_one_back(
        info,
        [v["head0"][0], head1[0]],
        (plan_proj, v["weights_proj"]),
        v["x_in"],
        v["grad_resid"],
        v["gain_one"],
        tok // 4,
    )
    v.update(head1=head1, tokens_low=tokens_low, gain_one_sum=gain_one_sum, up3=up3)
    v.update(there0=there0, far_h0=far_h0)
    sync()

    def place(out, parts, k, first):
        row = lax.rem(z - k + 4, 4)
        for j, part in enumerate(parts):
            at = (first + j) * part.shape[0]
            out = lax.dynamic_update_slice(out, part.astype(out.dtype)[None], (row, at, 0))
        return out

    v.update(out_one=v["one"])
    gathered = lax.all_gather(v["tokens_low"], "tp", axis=0, tiled=False)
    keep, send = weight_grad(
        v["normed_one_t"], [v["head0"][0], v["head1"][0]], v["grad_attn_t"], v["attended"]
    )
    gain_heads = v["head0"][1] + v["head1"][1]
    vector = jnp.concatenate(
        [
            natural(v["gain_one_sum"].reshape(4, quarter)).reshape(1, width),
            natural(v["gain_two_sum"].reshape(4, quarter)).reshape(1, width),
            gain_heads[:, 0].reshape(1, hd),
            gain_heads[:, 1].reshape(1, hd),
            jnp.sum(v["square"]).reshape(1, 1),
            jnp.zeros((1, 127), F32),
        ],
        axis=1,
    )
    vector = vector + core_swap(vector)
    v.update(keep=keep, send=send)
    v.update(vector=vector)
    sync()

    rows = quarter // 2
    flat = lambda a: a.reshape(4 * rows, a.shape[-1])
    attn_sums = [flat(p) for p in core_sum(info, v["keep"], core_swap(v["send"]))]
    vector = v["vector"] + x_swap(v["vector"])
    v.update(sums=attn_sums, vector=vector)
    sync()

    far_t = x_swap(v["sums"][3])
    part0 = summed([v["sum0"][0], v["far_h0"], v["there0"]], turned)
    ffn_sum = summed([part0, v["two_down"], v["up3"]], None, F32)
    vector = v["vector"] + y_swap(v["vector"])
    v.update(far_t=far_t, ffn_sum=ffn_sum, vector=vector)
    sync()

    far_h = x_swap(v["sums"][2])
    there = y_swap(summed([v["sums"][1], v["far_t"]]))
    output = jnp.zeros((rows_dev, tok, width), BF16)
    for k, parts in enumerate((v["results"], v["out_one"], v["out_two"], v["out_three"])):
        output = place(output, parts, k, 0)
    v.update(far_h=far_h, there=there, output=output)
    sync()

    parts = summed([v["sums"][0], v["far_h"], v["there"]])
    parts = [parts[k * rows : (k + 1) * rows] for k in range(4)]
    parts = [parts[0], z_down(parts[1]), z_far(parts[2]), z_up(parts[3])]
    ffn_other = y_swap(v["ffn_sum"])
    v.update(parts=parts)
    sync()

    attn_sum = summed(v["parts"], None, F32)
    vector = v["vector"] + lax.ppermute(v["vector"], "tp", Z_NEAR)
    v.update(attn_sum=attn_sum, vector=vector)
    v.update(ffn_other=ffn_other)
    sync()

    def finish(own, other):
        return jnp.concatenate(
            [jnp.where(ctx == 0, own, other), jnp.where(ctx == 0, other, own)], axis=0
        )

    def columns(first):
        parts = [ffn_grad[:, first(j) : first(j) + third] for j in range(3)]
        return jnp.concatenate(
            [
                jnp.where(ctx == 0, parts[0], parts[2]),
                parts[1],
                jnp.where(ctx == 0, parts[2], parts[0]),
            ],
            axis=1,
        )

    attn_other = y_swap(v["attn_sum"])
    vector = v["vector"] + lax.ppermute(v["vector"], "tp", Z_FAR)
    third = units // 3
    ffn_grad = finish(v["ffn_sum"], turn_chunks(v["ffn_other"]))
    grad_gate = columns(lambda j: 2 * j * third)
    grad_up = columns(lambda j: (2 * j + 1) * third)
    grad_down = columns(lambda j: 2 * units + j * third).T
    v.update(vector=vector, attn_other=attn_other)
    v.update(grad_gate=grad_gate, grad_up=grad_up, grad_down=grad_down)
    sync()

    tokens_grad = gathered.astype(F32)
    output = v["output"]
    sums_all = v["vector"][0]

    attn_grad = finish(v["attn_sum"], v["attn_other"])
    teacher_loss = sums_all[2 * width + 2 * hd] / (v["total_count"] * width)

    def own_part(at, size):
        return lax.dynamic_slice_in_dim(sums_all, at + fsdp * (size // 4), size // 4, 0)

    return (
        output,
        teacher_loss,
        tokens_grad,
        own_part(0, width),
        attn_grad[:, :q_cols],
        attn_grad[:, q_cols : q_cols + k_cols],
        attn_grad[:, q_cols + k_cols : proj],
        own_part(2 * width, hd),
        own_part(2 * width + hd, hd),
        attn_grad[:, proj:].T,
        own_part(width, width),
        v["grad_gate"],
        v["grad_up"],
        v["grad_down"],
    )


def solution(mesh):
    return jax.shard_map(
        per_device_rows if fits(mesh) else per_device_any,
        mesh=mesh,
        in_specs=(
            P("fsdp", "ctx", None),
            P("fsdp", "ctx", None),
            P("fsdp"),
            P("fsdp"),
            P("fsdp", "tp"),
            P("fsdp", "tp"),
            P("fsdp", "tp"),
            P("fsdp"),
            P("fsdp"),
            P("tp", "fsdp"),
            P("fsdp"),
            P("fsdp", "tp"),
            P("fsdp", "tp"),
            P("tp", "fsdp"),
        ),
        out_specs=(
            P("fsdp", "ctx", None),
            P(),
            P("fsdp", "ctx", None),
            P("fsdp"),
            P("fsdp", "tp"),
            P("fsdp", "tp"),
            P("fsdp", "tp"),
            P("fsdp"),
            P("fsdp"),
            P("tp", "fsdp"),
            P("fsdp"),
            P("fsdp", "tp"),
            P("fsdp", "tp"),
            P("tp", "fsdp"),
        ),
        check_vma=False,
    )
```

```python
import functools
import math

import jax
import jax.numpy as jnp
from jax import lax
from jax.experimental import pallas as pl
from jax.experimental.pallas import tpu as pltpu
from jax.sharding import PartitionSpec as P

EPS = 1e-05
THETA = 1000000.0
NEGATIVE = -1e30


def rms_scale(field_in, gain_vec):
    return (
        field_in * lax.rsqrt(jnp.mean(field_in * field_in, axis=-1, keepdims=True) + EPS) * gain_vec
    )


def rotate(field_in, positions):
    half_dim = field_in.shape[-1] // 2
    frequency = THETA ** (-(2.0 * jnp.arange(half_dim, dtype=jnp.float32)) / field_in.shape[-1])
    angles = positions[:, None] * frequency[None, :]
    cos_part = jnp.cos(angles)[:, None, :]
    sin_part = jnp.sin(angles)[:, None, :]
    lower_half = field_in[..., :half_dim]
    upper_half = field_in[..., half_dim:]
    return jnp.concatenate(
        [
            lower_half * cos_part - upper_half * sin_part,
            upper_half * cos_part + lower_half * sin_part,
        ],
        axis=-1,
    )


def linear(left_mat, right_mat):
    return jnp.dot(left_mat, right_mat, preferred_element_type=jnp.float32)


def linear_left(left_mat, right_mat):
    return lax.dot_general(
        left_mat, right_mat, (((0,), (0,)), ((), ())), preferred_element_type=jnp.float32
    )


def linear_right(left_mat, right_mat):
    return lax.dot_general(
        left_mat, right_mat, (((1,), (1,)), ((), ())), preferred_element_type=jnp.float32
    )


def swiglu(gate_act, up_act):
    return jax.nn.silu(gate_act) * up_act


def per_device_any(
    tokens,
    teacher,
    lengths,
    attn_gain,
    q_weight,
    k_weight,
    v_weight,
    q_gain,
    k_gain,
    o_weight,
    ffn_gain,
    gate_weight,
    up_weight,
    down_weight,
):
    (
        gain_one,
        w_query,
        w_key,
        w_value,
        gain_query,
        gain_key,
        w_output,
        gain_two,
        w_gate,
        w_upper,
        w_down,
    ) = (
        lax.all_gather(attn_gain, "fsdp", axis=0, tiled=True),
        lax.all_gather(q_weight, "fsdp", axis=0, tiled=True),
        lax.all_gather(k_weight, "fsdp", axis=0, tiled=True),
        lax.all_gather(v_weight, "fsdp", axis=0, tiled=True),
        lax.all_gather(q_gain, "fsdp", axis=0, tiled=True),
        lax.all_gather(k_gain, "fsdp", axis=0, tiled=True),
        lax.all_gather(o_weight, "fsdp", axis=1, tiled=True),
        lax.all_gather(ffn_gain, "fsdp", axis=0, tiled=True),
        lax.all_gather(gate_weight, "fsdp", axis=0, tiled=True),
        lax.all_gather(up_weight, "fsdp", axis=0, tiled=True),
        lax.all_gather(down_weight, "fsdp", axis=1, tiled=True),
    )
    rows_dev, block_len, model_width = tokens.shape
    count_tok = rows_dev * block_len
    head_dim = gain_query.shape[0]
    q_heads = w_query.shape[1] // head_dim
    kv_heads = w_key.shape[1] // head_dim
    group_size = q_heads // kv_heads
    score_scale = head_dim ** (-0.5)
    row_len = block_len * lax.axis_size("ctx")
    key_block = math.gcd(row_len, 512)
    block_start = lax.axis_index("ctx") * block_len
    tiles_used = (block_start + block_len + key_block - 1) // key_block
    slot_pos = block_start + jnp.arange(block_len, dtype=jnp.int32)
    positions = slot_pos.astype(jnp.float32)
    valid = (slot_pos[None, :] < lengths[:, None]).astype(jnp.float32)
    slots = count_tok * lax.axis_size("fsdp") * lax.axis_size("ctx")
    gain_two_f = gain_two.astype(jnp.float32)
    gain_one_f = gain_one.astype(jnp.float32)
    inputs = tokens.astype(jnp.float32)
    normed_one, back_one = jax.vjp(rms_scale, inputs, gain_one_f)
    normed_low = normed_one.astype(jnp.bfloat16).reshape(count_tok, model_width)
    query_raw = linear(normed_low, w_query)
    key_raw = linear(normed_low, w_key)
    value_raw = linear(normed_low, w_value)

    def heads_post(raw_heads, gain_vec):
        shaped = raw_heads.reshape(rows_dev, block_len, -1, head_dim)
        return rotate(rms_scale(shaped, gain_vec), positions)

    query_rot, query_back = jax.vjp(heads_post, query_raw, gain_query.astype(jnp.float32))
    key_rot, key_back = jax.vjp(heads_post, key_raw, gain_key.astype(jnp.float32))
    queries = query_rot.astype(jnp.bfloat16).reshape(
        rows_dev, block_len, kv_heads, group_size, head_dim
    )
    key_rows = key_rot.astype(jnp.bfloat16).reshape(rows_dev, block_len, kv_heads * head_dim)
    values = value_raw.astype(jnp.bfloat16).reshape(rows_dev, block_len, kv_heads * head_dim)
    keys_all, values_all = (
        lax.all_gather(key_rows, "ctx", axis=1, tiled=True),
        lax.all_gather(values, "ctx", axis=1, tiled=True),
    )

    def key_tile(tile_index):
        tile_start = tile_index * key_block
        key_pos = tile_start + jnp.arange(key_block, dtype=jnp.int32)
        key_part = lax.dynamic_slice_in_dim(keys_all, tile_start, key_block, 1).reshape(
            rows_dev, key_block, kv_heads, head_dim
        )
        value_part = lax.dynamic_slice_in_dim(values_all, tile_start, key_block, 1).reshape(
            rows_dev, key_block, kv_heads, head_dim
        )
        scores = (
            jnp.einsum("rqhgd,rkhd->rhgqk", queries, key_part, preferred_element_type=jnp.float32)
            * score_scale
        )
        allowed = (key_pos[None, None, :] <= slot_pos[None, :, None]) & (
            key_pos[None, None, :] < lengths[:, None, None]
        )
        return (tile_start, scores, allowed[:, None, None], key_part, value_part)

    stat_shape = (rows_dev, kv_heads, group_size, block_len)

    def stats_step(tile_index, carried):
        running_max, running_sum = carried
        tile_start, scores, allowed, key_part, value_part = key_tile(tile_index)
        masked = jnp.where(allowed, scores, NEGATIVE)
        new_max = jnp.maximum(running_max, jnp.max(masked, axis=-1))
        terms = jnp.where(allowed, jnp.exp(masked - new_max[..., None]), 0.0)
        return (new_max, running_sum * jnp.exp(running_max - new_max) + jnp.sum(terms, axis=-1))

    running_max, running_sum = lax.fori_loop(
        0,
        tiles_used,
        stats_step,
        (jnp.full(stat_shape, NEGATIVE, jnp.float32), jnp.zeros(stat_shape, jnp.float32)),
    )
    log_total = running_max + jnp.log(running_sum)
    out_shape = (rows_dev, block_len, kv_heads, group_size, head_dim)

    def value_step(tile_index, carried):
        rounded_out, exact_out = carried
        tile_start, scores, allowed, key_part, value_part = key_tile(tile_index)
        tile_probs = jnp.where(allowed, jnp.exp(scores - log_total[..., None]), 0.0)
        rounded_out = rounded_out + jnp.einsum(
            "rhgqk,rkhd->rqhgd",
            tile_probs.astype(jnp.bfloat16),
            value_part,
            preferred_element_type=jnp.float32,
        )
        exact_out = exact_out + jnp.einsum(
            "rhgqk,rkhd->rqhgd", tile_probs, value_part.astype(jnp.float32)
        )
        return (rounded_out, exact_out)

    rounded_out, exact_out = lax.fori_loop(
        0,
        tiles_used,
        value_step,
        (jnp.zeros(out_shape, jnp.float32), jnp.zeros(out_shape, jnp.float32)),
    )
    attended = rounded_out.astype(jnp.bfloat16).reshape(count_tok, q_heads * head_dim)
    attn_total = lax.psum(linear(attended, w_output), "tp")
    resid = inputs + attn_total.reshape(rows_dev, block_len, model_width)
    normed_two, back_two = jax.vjp(rms_scale, resid, gain_two_f)
    normed_second = normed_two.astype(jnp.bfloat16).reshape(count_tok, model_width)
    gate_act = linear(normed_second, w_gate)
    up_act = linear(normed_second, w_upper)
    hidden_full, back_glu = jax.vjp(swiglu, gate_act, up_act)
    hidden = hidden_full.astype(jnp.bfloat16)
    ffn_total = lax.psum(linear(hidden, w_down), "tp")
    result = resid + ffn_total.reshape(rows_dev, block_len, model_width)
    error_value = result - teacher.astype(jnp.float32)
    valid_col = valid[..., None]
    total_square, total_count = lax.psum(
        (jnp.sum(valid_col * error_value * error_value), jnp.sum(valid)), ("fsdp", "ctx")
    )
    teacher_loss = total_square / (total_count * model_width)
    grad_result = valid_col * error_value * (slots / total_count)
    grad_low = grad_result.astype(jnp.bfloat16).reshape(count_tok, model_width)
    grad_down = linear_left(hidden, grad_low)
    grad_hidden = linear_right(grad_low, w_down)
    grad_gate_full, grad_up_full = back_glu(grad_hidden)
    grad_gate = grad_gate_full.astype(jnp.bfloat16)
    grad_up = grad_up_full.astype(jnp.bfloat16)
    grad_wgate = linear_left(normed_second, grad_gate)
    grad_wup = linear_left(normed_second, grad_up)
    normed_two_part = linear_right(grad_gate, w_gate) + linear_right(grad_up, w_upper)
    grad_normed_two = lax.psum(normed_two_part, "tp")
    grad_resid_norm, grad_gain_two = back_two(
        grad_normed_two.reshape(rows_dev, block_len, model_width)
    )
    grad_resid = grad_result + grad_resid_norm
    grad_attn_low = grad_resid.astype(jnp.bfloat16).reshape(count_tok, model_width)
    grad_woutput = linear_left(attended, grad_attn_low)
    grad_attended = linear_right(grad_attn_low, w_output).astype(jnp.bfloat16).reshape(out_shape)
    delta = jnp.einsum("rqhgd,rqhgd->rhgq", grad_attended.astype(jnp.float32), exact_out)
    full_shape = (rows_dev, row_len, kv_heads * head_dim)

    def grad_step(tile_index, carried):
        grad_queries, grad_keys, grad_values = carried
        tile_start, scores, allowed, key_part, value_part = key_tile(tile_index)
        tile_probs = jnp.where(allowed, jnp.exp(scores - log_total[..., None]), 0.0)
        grad_probs = jnp.einsum(
            "rqhgd,rkhd->rhgqk", grad_attended, value_part, preferred_element_type=jnp.float32
        )
        grad_scores = (tile_probs * (grad_probs - delta[..., None])).astype(jnp.bfloat16)
        grad_queries = (
            grad_queries
            + jnp.einsum(
                "rhgqk,rkhd->rqhgd", grad_scores, key_part, preferred_element_type=jnp.float32
            )
            * score_scale
        )
        key_term = (
            jnp.einsum(
                "rhgqk,rqhgd->rkhd", grad_scores, queries, preferred_element_type=jnp.float32
            )
            * score_scale
        )
        value_term = jnp.einsum(
            "rhgqk,rqhgd->rkhd",
            tile_probs.astype(jnp.bfloat16),
            grad_attended,
            preferred_element_type=jnp.float32,
        )
        grad_keys = lax.dynamic_update_slice_in_dim(
            grad_keys, key_term.reshape(rows_dev, key_block, kv_heads * head_dim), tile_start, 1
        )
        grad_values = lax.dynamic_update_slice_in_dim(
            grad_values, value_term.reshape(rows_dev, key_block, kv_heads * head_dim), tile_start, 1
        )
        return (grad_queries, grad_keys, grad_values)

    grad_queries, grad_keys, grad_values = lax.fori_loop(
        0,
        tiles_used,
        grad_step,
        (
            jnp.zeros(out_shape, jnp.float32),
            jnp.zeros(full_shape, jnp.float32),
            jnp.zeros(full_shape, jnp.float32),
        ),
    )
    key_grad, value_grad = (
        lax.psum_scatter(grad_keys, "ctx", scatter_dimension=1, tiled=True),
        lax.psum_scatter(grad_values, "ctx", scatter_dimension=1, tiled=True),
    )
    grad_query_raw, grad_gain_query = query_back(
        grad_queries.reshape(rows_dev, block_len, q_heads, head_dim)
    )
    grad_key_raw, grad_gain_key = key_back(
        key_grad.reshape(rows_dev, block_len, kv_heads, head_dim)
    )
    query_low = grad_query_raw.astype(jnp.bfloat16)
    key_low = grad_key_raw.astype(jnp.bfloat16)
    value_low = value_grad.reshape(count_tok, kv_heads * head_dim).astype(jnp.bfloat16)
    grad_wquery = linear_left(normed_low, query_low)
    grad_wkey = linear_left(normed_low, key_low)
    grad_wvalue = linear_left(normed_low, value_low)
    normed_part = (
        linear_right(query_low, w_query)
        + linear_right(key_low, w_key)
        + linear_right(value_low, w_value)
    )
    grad_normed_one, grad_gain_query, grad_gain_key = lax.psum(
        (normed_part, grad_gain_query, grad_gain_key), "tp"
    )
    grad_input_norm, grad_gain_one = back_one(
        grad_normed_one.reshape(rows_dev, block_len, model_width)
    )
    tokens_grad = grad_resid + grad_input_norm
    partials = (
        grad_gain_one,
        grad_wquery,
        grad_wkey,
        grad_wvalue,
        grad_gain_query,
        grad_gain_key,
        grad_woutput,
        grad_gain_two,
        grad_wgate,
        grad_wup,
        grad_down,
    )
    pieces = (
        lax.psum_scatter(partials[0], ("fsdp", "ctx"), scatter_dimension=0, tiled=True),
        lax.psum_scatter(partials[1], ("fsdp", "ctx"), scatter_dimension=0, tiled=True),
        lax.psum_scatter(partials[2], ("fsdp", "ctx"), scatter_dimension=0, tiled=True),
        lax.psum_scatter(partials[3], ("fsdp", "ctx"), scatter_dimension=0, tiled=True),
        lax.psum_scatter(partials[4], ("fsdp", "ctx"), scatter_dimension=0, tiled=True),
        lax.psum_scatter(partials[5], ("fsdp", "ctx"), scatter_dimension=0, tiled=True),
        lax.psum_scatter(partials[6], ("fsdp", "ctx"), scatter_dimension=1, tiled=True),
        lax.psum_scatter(partials[7], ("fsdp", "ctx"), scatter_dimension=0, tiled=True),
        lax.psum_scatter(partials[8], ("fsdp", "ctx"), scatter_dimension=0, tiled=True),
        lax.psum_scatter(partials[9], ("fsdp", "ctx"), scatter_dimension=0, tiled=True),
        lax.psum_scatter(partials[10], ("fsdp", "ctx"), scatter_dimension=1, tiled=True),
    )
    summed = (
        lax.all_gather(pieces[0], "ctx", axis=0, tiled=True),
        lax.all_gather(pieces[1], "ctx", axis=0, tiled=True),
        lax.all_gather(pieces[2], "ctx", axis=0, tiled=True),
        lax.all_gather(pieces[3], "ctx", axis=0, tiled=True),
        lax.all_gather(pieces[4], "ctx", axis=0, tiled=True),
        lax.all_gather(pieces[5], "ctx", axis=0, tiled=True),
        lax.all_gather(pieces[6], "ctx", axis=1, tiled=True),
        lax.all_gather(pieces[7], "ctx", axis=0, tiled=True),
        lax.all_gather(pieces[8], "ctx", axis=0, tiled=True),
        lax.all_gather(pieces[9], "ctx", axis=0, tiled=True),
        lax.all_gather(pieces[10], "ctx", axis=1, tiled=True),
    )
    return (
        result.astype(jnp.bfloat16),
        teacher_loss,
        tokens_grad,
        summed[0],
        summed[1],
        summed[2],
        summed[3],
        summed[4],
        summed[5],
        summed[6],
        summed[7],
        summed[8],
        summed[9],
        summed[10],
    )


BF16 = jnp.bfloat16
F32 = jnp.float32
LOG2E = math.log2(math.e)
X_SWAP = [(0, 2), (2, 0), (1, 3), (3, 1)]
CORE_SWAP = [(0, 1), (1, 0), (2, 3), (3, 2)]
Y_SWAP = [(0, 1), (1, 0)]
Z_UP = [(0, 1), (1, 2), (2, 3), (3, 0)]
Z_DOWN = [(0, 3), (1, 0), (2, 1), (3, 2)]
Z_NEAR = [(0, 1), (1, 0), (2, 3), (3, 2)]
Z_FAR = [(0, 2), (2, 0), (1, 3), (3, 1)]
MASKS = (0, 2, 1, 3)
ANY = pl.BlockSpec(memory_space=pl.ANY)
SMEM = pl.BlockSpec(memory_space=pltpu.SMEM)


def fits(mesh):
    return dict(mesh.shape) == {"fsdp": 4, "ctx": 2, "tp": 4}


def dot(left, right, left_dim, right_dim):
    return lax.dot_general(
        left, right, (((left_dim,), (right_dim,)), ((), ())), preferred_element_type=F32
    )


def sigmoid(v):
    return 0.5 * jnp.tanh(0.5 * v) + 0.5


def whole(shape):
    zeros = (0,) * len(shape)
    return pl.BlockSpec(shape, lambda *_: zeros, pipeline_mode=pl.Buffered(1))


def settings(dims, mib):
    return pltpu.CompilerParams(
        dimension_semantics=("arbitrary",) * dims, vmem_limit_bytes=mib << 20
    )


def shape_of(shape, dtype):
    return jax.ShapeDtypeStruct(shape, dtype)


def cost(large, microseconds=None):
    size = 1 << 42 if large else 1 << 10
    if microseconds is not None:
        size = int(microseconds * 1.15e9)
    return pl.CostEstimate(flops=size, bytes_accessed=size >> 12, transcendentals=0)


def pack_kernel(info, o_in, g_in, u_in, d_in, *refs):
    out_ref, ffn_ref, *chunk_refs, others_ref, o_ref, g_ref, u_ref, d_ref, sems = refs
    ctx = info[2]
    pairs = ((o_in, o_ref), (g_in, g_ref), (u_in, u_ref), (d_in, d_ref))
    copies = [pltpu.make_async_copy(a, b, sems.at[i]) for i, (a, b) in enumerate(pairs)]
    for copy in copies:
        copy.start()
    for copy in copies:
        copy.wait()
    out_ref[...] = o_ref[...].astype(F32).T.astype(BF16)
    third = g_ref.shape[1] // 3
    for j in range(3):
        at = pl.multiple_of(jnp.where(ctx == 0, j, 2 - j) * third, third)
        parts = [
            g_ref[:, pl.ds(at, third)],
            u_ref[:, pl.ds(at, third)],
            d_ref[pl.ds(at, third), :].astype(F32).T.astype(BF16),
        ]
        for i, part in enumerate(parts):
            chunk_refs[j][:, i * third : (i + 1) * third] = part
            if j:
                others_ref[:, (3 * j - 3 + i) * third : (3 * j - 2 + i) * third] = part
            ffn_ref[:, (3 * j + i) * third : (3 * j + i + 1) * third] = part


def pack(info, o, g, u, d):
    rows, units = g.shape
    feats = o.shape[0]
    widths = (feats, 3 * units, units, units, units, 2 * units)
    return pl.pallas_call(
        pack_kernel,
        in_specs=[SMEM] + [ANY] * 4,
        out_specs=[pl.BlockSpec(memory_space=pltpu.VMEM)] * 6,
        out_shape=[shape_of((rows, n), BF16) for n in widths],
        scratch_shapes=[pltpu.VMEM(a.shape, BF16) for a in (o, g, u, d)]
        + [pltpu.SemaphoreType.DMA((4,))],
        compiler_params=pltpu.CompilerParams(vmem_limit_bytes=24 << 20),
        cost_estimate=cost(False),
        name="pack",
    )(info, o, g, u, d)


def join_kernel(q_ref, k_ref, v_ref, out_ref):
    at = 0
    for ref in (q_ref, k_ref, v_ref):
        out_ref[:, at : at + ref.shape[1]] = ref[...]
        at += ref.shape[1]


def join(q, k, v):
    return pl.pallas_call(
        join_kernel,
        out_shape=shape_of((q.shape[0], q.shape[1] + k.shape[1] + v.shape[1]), BF16),
        compiler_params=pltpu.CompilerParams(vmem_limit_bytes=8 << 20),
        cost_estimate=cost(False),
        name="join",
    )(q, k, v)


def norm_one_kernel(info, tok_ref, gain_ref, x_ref, nt_ref, x32):
    quarter = x_ref.shape[1] // 4
    for p, mask in enumerate(MASKS):
        at = pl.multiple_of(jnp.bitwise_xor(info[1], mask) * quarter, quarter)
        part = tok_ref[0, :, pl.ds(at, quarter)]
        x_ref[:, p * quarter : (p + 1) * quarter] = part
        x32[:, p * quarter : (p + 1) * quarter] = part.astype(F32)
    x = x32[...]
    rho = lax.rsqrt(jnp.mean(x * x, axis=-1, keepdims=True) + EPS)
    nt_ref[...] = (x * rho * gain_ref[...]).T.astype(BF16)


def norm_one(info, tokens, gain, tile):
    _, tok, width = tokens.shape
    return pl.pallas_call(
        norm_one_kernel,
        grid_spec=pltpu.PrefetchScalarGridSpec(
            num_scalar_prefetch=1,
            grid=(tok // tile,),
            in_specs=[
                pl.BlockSpec((1, tile, width), lambda i, info: (info[0], i, 0)),
                pl.BlockSpec((1, width), lambda i, info: (0, 0)),
            ],
            out_specs=[
                pl.BlockSpec((tile, width), lambda i, info: (i, 0)),
                pl.BlockSpec((width, tile), lambda i, info: (0, i)),
            ],
            scratch_shapes=[pltpu.VMEM((tile, width), F32)],
        ),
        out_shape=[shape_of((tok, width), BF16), shape_of((width, tok), BF16)],
        compiler_params=settings(1, 24),
        cost_estimate=cost(False),
        name="norm_one",
    )(info, tokens, gain)


def proj_kernel(heads, block, plan, count, info, *refs):
    nt_ref, cos_ref, sin_ref, qg_ref, kg_ref, rot_ref, raw_ref, w_ref, sem = refs[count:]
    rows = w_ref.shape[0] // 4

    @pl.when(pl.program_id(0) == 0)
    def _():
        for k in range(4):

            @pl.when(block(info) == k)
            def _():
                for p, (piece, row) in enumerate(plan[k]):
                    src = refs[piece].at[pl.ds(row, rows)]
                    pltpu.make_async_copy(src, w_ref.at[pl.ds(p * rows, rows)], sem).start()

        pltpu.make_async_copy(w_ref, w_ref, sem).wait()

    hd = qg_ref.shape[0]
    half = hd // 2
    raw = dot(w_ref[...], nt_ref[...], 0, 0)
    cos_part, sin_part = cos_ref[...], sin_ref[...]
    heads_q, heads_k = heads
    raw_ref[...] = raw.astype(BF16)
    for h in range(heads_q + heads_k):
        v = raw[h * hd : (h + 1) * hd]
        rho = lax.rsqrt(jnp.mean(v * v, axis=0, keepdims=True) + EPS)
        v = v * rho * (qg_ref[...] if h < heads_q else kg_ref[...])
        a, b = v[:half], v[half:]
        rot_ref[h * hd : h * hd + half, :] = (a * cos_part - b * sin_part).astype(BF16)
        rot_ref[h * hd + half : (h + 1) * hd, :] = (b * cos_part + a * sin_part).astype(BF16)
    at = (heads_q + heads_k) * hd
    rot_ref[at:, :] = raw[at:].astype(BF16)


def project(info, weights, normed_t, cos_part, sin_part, gain_q, gain_k, heads, block):
    plan, pieces = weights
    width, tok = normed_t.shape
    cols = pieces[0].shape[1]
    tile = min(512, tok)
    const = lambda a: pl.BlockSpec(a.shape, lambda i, info: (0, 0))
    tab = lambda a: pl.BlockSpec((a.shape[0], tile), lambda i, info: (0, i))
    return pl.pallas_call(
        functools.partial(proj_kernel, heads, block, plan, len(pieces)),
        grid_spec=pltpu.PrefetchScalarGridSpec(
            num_scalar_prefetch=1,
            grid=(tok // tile,),
            in_specs=[ANY] * len(pieces)
            + [tab(normed_t), tab(cos_part), tab(sin_part), const(gain_q), const(gain_k)],
            out_specs=[pl.BlockSpec((cols, tile), lambda i, info: (0, i))] * 2,
            scratch_shapes=[pltpu.VMEM((width, cols), BF16), pltpu.SemaphoreType.DMA],
        ),
        out_shape=[shape_of((cols, tok), BF16), shape_of((cols, tok), BF16)],
        compiler_params=settings(1, 24),
        cost_estimate=cost(False),
        name="project",
    )(info, *pieces, normed_t, cos_part, sin_part, gain_q, gain_k)


def head_back_kernel(
    heads, info, dm_ref, dt_ref, rm_ref, rt_ref, cos_ref, sin_ref, qg_ref, kg_ref, out_ref, gg_ref
):
    step, part = pl.program_id(0), pl.program_id(1)
    hd = qg_ref.shape[0]
    half = hd // 2
    heads_q, heads_k = heads
    cos_part, sin_part = cos_ref[...], sin_ref[...]
    tile = cos_part.shape[1]

    @pl.when((step == 0) & (part == 0))
    def _():
        gg_ref[...] = jnp.zeros_like(gg_ref)

    def work(d_ref, r_ref):
        gain_q = jnp.zeros((hd, 1), F32)
        gain_k = jnp.zeros((hd, 1), F32)
        done = []
        for h in range(heads_q + heads_k):
            is_q = h < heads_q
            g = d_ref[h * hd : (h + 1) * hd, :].astype(F32)
            raw = r_ref[h * hd : (h + 1) * hd, :].astype(F32)
            a, b = g[:half], g[half:]
            turned = jnp.concatenate(
                [a * cos_part + b * sin_part, b * cos_part - a * sin_part], axis=0
            )
            rho = lax.rsqrt(jnp.mean(raw * raw, axis=0, keepdims=True) + EPS)
            unit = raw * rho
            prod = turned * unit
            scaled = turned * (qg_ref[...] if is_q else kg_ref[...])
            mean = jnp.mean(scaled * unit, axis=0, keepdims=True)
            done.append(rho * (scaled - unit * mean))
            total = jnp.sum(prod, axis=1, keepdims=True)
            if is_q:
                gain_q = gain_q + total
            else:
                gain_k = gain_k + total
        done.append(d_ref[(heads_q + heads_k) * hd :, :].astype(F32))
        out_ref[0] = jnp.concatenate(done, axis=0).T.astype(BF16)
        lane = lax.broadcasted_iota(jnp.int32, gg_ref.shape, 1)
        gg_ref[...] += jnp.where(lane == 0, gain_q, jnp.where(lane == 1, gain_k, 0.0))

    @pl.when(step == 0)
    def _():
        work(dm_ref, rm_ref)

    @pl.when(step == 1)
    def _():
        work(dt_ref, rt_ref)


def head_back(info, grad_mine, grad_theirs, raw_mine, raw_theirs, cos_part, sin_part, gq, gk, heads):
    cols, tok = grad_mine.shape
    tile = min(512, tok)
    mine = pl.BlockSpec((cols, tile), lambda s, i, info: (0, jnp.where(s == 0, i, tok // tile - 1)))
    theirs = pl.BlockSpec((cols, tile), lambda s, i, info: (0, jnp.where(s == 0, 0, i)))
    tab = lambda a: pl.BlockSpec((a.shape[0], tile), lambda s, i, info: (0, i))
    const = lambda a: pl.BlockSpec(a.shape, lambda s, i, info: (0, 0))
    return pl.pallas_call(
        functools.partial(head_back_kernel, heads),
        grid_spec=pltpu.PrefetchScalarGridSpec(
            num_scalar_prefetch=1,
            grid=(2, tok // tile),
            in_specs=[
                mine,
                theirs,
                mine,
                theirs,
                tab(cos_part),
                tab(sin_part),
                const(gq),
                const(gk),
            ],
            out_specs=[
                pl.BlockSpec(
                    (1, tile, cols), lambda s, i, info: (jnp.bitwise_xor(info[2], s), i, 0)
                ),
                pl.BlockSpec((gq.shape[0], 128), lambda s, i, info: (0, 0)),
            ],
        ),
        out_shape=[shape_of((2, tok, cols), BF16), shape_of((gq.shape[0], 128), F32)],
        compiler_params=settings(2, 60),
        cost_estimate=cost(False),
        name="head_back",
    )(info, grad_mine, grad_theirs, raw_mine, raw_theirs, cos_part, sin_part, gq, gk)


def load_rows(info, mine_ref, got_ref, rows, sems):
    tok = mine_ref.shape[1]
    ctx = info[2]
    here = pl.multiple_of(ctx * tok, tok)
    there = pl.multiple_of((1 - ctx) * tok, tok)
    one = pltpu.make_async_copy(mine_ref, rows.at[:, pl.ds(here, tok)], sems.at[0])
    two = pltpu.make_async_copy(got_ref, rows.at[:, pl.ds(there, tok)], sems.at[1])
    one.start()
    two.start()
    one.wait()
    two.wait()


def keys_with_bias(keys, length):
    hd, slots = keys.shape
    pos = lax.broadcasted_iota(jnp.int32, (hd, slots), 1)
    row = lax.broadcasted_iota(jnp.int32, (hd, slots), 0)
    bias = jnp.where((row == 0) & (pos >= length), NEGATIVE, 0.0)
    return jnp.concatenate([keys.astype(F32), bias], axis=0).T.astype(BF16)


def query_with_one(pair):
    one_row = jnp.where(lax.broadcasted_iota(jnp.int32, pair.shape, 0) == 0, 1.0, 0.0)
    return jnp.concatenate([pair, one_row.astype(BF16)], axis=0)


def by_halves(left, right):
    half = left.shape[1] // 2
    return jnp.concatenate(
        [left[:, :half], right[:, :half], left[:, half:], right[:, half:]], axis=1
    )


def by_heads(both):
    quarter = both.shape[1] // 4
    part = lambda i: both[:, i * quarter : (i + 1) * quarter]
    return (
        jnp.concatenate([part(0), part(2)], axis=1),
        jnp.concatenate([part(1), part(3)], axis=1),
    )


def causal(scores):
    half = scores.shape[0]
    key_pos = lax.broadcasted_iota(jnp.int32, (half, half), 0)
    query_pos = lax.broadcasted_iota(jnp.int32, (half, half), 1)
    allowed = key_pos <= query_pos
    return jnp.where(jnp.concatenate([allowed, allowed], axis=1), scores, NEGATIVE)


def attn_fwd_kernel(
    width, hd, info, mine_ref, got_ref, keep_ref, send_ref, lse_ref, rows, key_rows, sems
):
    head, block = pl.program_id(0), pl.program_id(1)
    heads_k = pl.num_programs(0)
    scale = hd**-0.5 * LOG2E
    length = info[3]
    key_at = pl.multiple_of(heads_k * 2 * hd + head * hd, hd)
    value_at = pl.multiple_of(heads_k * 3 * hd + head * hd, hd)
    query_at = pl.multiple_of(head * 2 * hd, 2 * hd)

    @pl.when((head == 0) & (block == 0))
    def _():
        load_rows(info, mine_ref, got_ref, rows, sems)

    @pl.when(block == 0)
    def _():
        key_rows[...] = keys_with_bias(rows[pl.ds(key_at, hd), :], length)

    start = pl.multiple_of(block * width, width)
    both = rows[pl.ds(query_at, 2 * hd), pl.ds(start, width)]
    query = query_with_one(by_halves(both[:hd], both[hd:]))

    def tile(at, carried, diagonal):
        out, total = carried
        scores = dot(key_rows[pl.ds(at, width), :], query, 1, 0)
        if diagonal:
            key_pos = lax.broadcasted_iota(jnp.int32, (width, width), 0)
            query_pos = lax.broadcasted_iota(jnp.int32, (width, width), 1)
            allowed = key_pos <= query_pos
            allowed = by_halves(allowed, allowed)
            scores = jnp.where(allowed, scores, NEGATIVE)
        probs = jnp.exp2(scores * scale)
        total = total + jnp.sum(probs, axis=0, keepdims=True)
        out = out + dot(rows[pl.ds(value_at, hd), pl.ds(at, width)], probs.astype(BF16), 1, 0)
        return out, total

    carried = (jnp.zeros((hd, 2 * width), F32), jnp.zeros((1, 2 * width), F32))
    full = jnp.minimum(block, lax.div(length + width - 1, width))
    carried = lax.fori_loop(
        0, full, lambda j, c: tile(pl.multiple_of(j * width, width), c, False), carried
    )
    out, total = tile(start, carried, True)
    out = out * (1.0 / total)
    out = jnp.concatenate(by_heads(out), axis=0).T.astype(BF16)
    here = block // 2 == info[2]

    @pl.when(here)
    def _():
        keep_ref[...] = out

    @pl.when(jnp.logical_not(here))
    def _():
        send_ref[...] = out

    log_first, log_second = by_heads(jnp.log2(total))
    lse_ref[0, 0:1, :] = log_first
    lse_ref[0, 1:2, :] = log_second


def keep_block(i, info):
    return jnp.clip(i - 2 * info[2], 0, 1)


def send_block(i, info):
    return jnp.clip(i - 2 * (1 - info[2]), 0, 1)


def attn_fwd(info, mine, got, hd):
    cols, tok = mine.shape
    heads_k = cols // (4 * hd)
    width = tok // 2
    return pl.pallas_call(
        functools.partial(attn_fwd_kernel, width, hd),
        grid_spec=pltpu.PrefetchScalarGridSpec(
            num_scalar_prefetch=1,
            grid=(heads_k, 4),
            in_specs=[ANY, ANY],
            out_specs=[
                pl.BlockSpec((width, 2 * hd), lambda h, i, info: (keep_block(i, info), h)),
                pl.BlockSpec((width, 2 * hd), lambda h, i, info: (send_block(i, info), h)),
                pl.BlockSpec((1, 2, width), lambda h, i, info: (h, 0, i)),
            ],
            scratch_shapes=[
                pltpu.VMEM((cols, 2 * tok), BF16),
                pltpu.VMEM((2 * tok, 2 * hd), BF16),
                pltpu.SemaphoreType.DMA((2,)),
            ],
        ),
        out_shape=[
            shape_of((tok, heads_k * 2 * hd), BF16),
            shape_of((tok, heads_k * 2 * hd), BF16),
            shape_of((heads_k, 2, 2 * tok), F32),
        ],
        compiler_params=settings(2, 60),
        cost_estimate=cost(True),
        name="attn_fwd",
    )(info, mine, got)


def attn_bwd_kernel(
    width,
    hd,
    info,
    mine_ref,
    got_ref,
    ok_ref,
    os_ref,
    gk_ref,
    gs_ref,
    lse_ref,
    keep_ref,
    send_ref,
    rows,
    key_rows,
    value_rows,
    key_sum,
    value_sum,
    sems,
):
    head, block = pl.program_id(0), pl.program_id(1)
    heads_k = pl.num_programs(0)
    scale = hd**-0.5
    length = info[3]
    ctx = info[2]
    tok = keep_ref.shape[1]
    key_at = pl.multiple_of(heads_k * 2 * hd + head * hd, hd)
    value_at = pl.multiple_of(heads_k * 3 * hd + head * hd, hd)
    query_at = pl.multiple_of(head * 2 * hd, 2 * hd)

    @pl.when((head == 0) & (block == 0))
    def _():
        load_rows(info, mine_ref, got_ref, rows, sems)

    @pl.when(block == 0)
    def _():
        key_rows[...] = keys_with_bias(rows[pl.ds(key_at, hd), :], length)
        value_rows[...] = rows[pl.ds(value_at, hd), :].astype(F32).T.astype(BF16)
        key_sum[...] = jnp.zeros_like(key_sum)
        value_sum[...] = jnp.zeros_like(value_sum)

    start = pl.multiple_of(block * width, width)
    here = block // 2 == ctx

    def store_query(value):
        at = pl.ds(pl.multiple_of((block % 2) * width, width), width)

        @pl.when(here)
        def _():
            keep_ref[pl.ds(query_at, 2 * hd), at] = value

        @pl.when(jnp.logical_not(here))
        def _():
            send_ref[pl.ds(query_at, 2 * hd), at] = value

    @pl.when(block * width < length)
    def _():
        both = rows[pl.ds(query_at, 2 * hd), pl.ds(start, width)]
        pair = by_halves(both[:hd], both[hd:])
        query = query_with_one(pair)
        query_rows = pair.astype(F32).T.astype(BF16)
        grad_wide = jnp.where(here, gk_ref[...].astype(F32), gs_ref[...].astype(F32))
        out_wide = jnp.where(here, ok_ref[...].astype(F32), os_ref[...].astype(F32))
        grad_t = grad_wide.T
        prod = (grad_wide * out_wide).T
        grad = by_halves(grad_t[:hd], grad_t[hd:]).astype(BF16)
        half = width // 2
        grad_rows = jnp.concatenate(
            [
                grad_wide[:half, :hd],
                grad_wide[:half, hd:],
                grad_wide[half:, :hd],
                grad_wide[half:, hd:],
            ],
            axis=0,
        ).astype(BF16)
        delta = by_halves(
            jnp.sum(prod[:hd], axis=0, keepdims=True), jnp.sum(prod[hd:], axis=0, keepdims=True)
        )
        lse = by_halves(lse_ref[0, 0:1, :], lse_ref[0, 1:2, :])

        def terms(at, keys, first, mask):
            scores = dot(key_rows[pl.ds(at, keys), :], query[:, first:], 1, 0)
            if mask:
                part = causal(scores[:, :width])
                wide = scores.shape[1] > width
                scores = jnp.concatenate([part, scores[:, width:]], axis=1) if wide else part
            probs = jnp.exp2(scores * (scale * LOG2E) - lse[:, first:])
            grad_probs = dot(value_rows[pl.ds(at, keys), :], grad[:, first:], 1, 0)
            grad_scores = (probs * (grad_probs - delta[:, first:])).astype(BF16)
            value_sum[pl.ds(at, keys), :] += dot(probs.astype(BF16), grad_rows[first:], 1, 0)
            key_sum[pl.ds(at, keys), :] += dot(grad_scores, query_rows[first:], 1, 0)
            return dot(rows[pl.ds(key_at, hd), pl.ds(at, keys)], grad_scores, 1, 0)

        query_sum = lax.fori_loop(
            0,
            block,
            lambda j, s: s + terms(pl.multiple_of(j * width, width), width, 0, False),
            jnp.zeros((hd, 2 * width), F32),
        )
        query_sum = query_sum + terms(start, half, 0, True)
        later = terms(pl.multiple_of(start + half, half), half, width, True)
        query_sum = jnp.concatenate([query_sum[:, :width], query_sum[:, width:] + later], axis=1)
        store_query(jnp.concatenate(by_heads(query_sum * scale), axis=0).astype(BF16))

    @pl.when(block * width >= length)
    def _():
        store_query(jnp.zeros((2 * hd, width), BF16))

    @pl.when(block == 3)
    def _():
        for at, total in ((key_at, key_sum[...] * scale), (value_at, value_sum[...])):
            total = total.T.astype(BF16)
            left, right = total[:, :tok], total[:, tok:]

            @pl.when(ctx == 0)
            def _():
                keep_ref[pl.ds(at, hd), :] = left
                send_ref[pl.ds(at, hd), :] = right

            @pl.when(ctx == 1)
            def _():
                keep_ref[pl.ds(at, hd), :] = right
                send_ref[pl.ds(at, hd), :] = left


def attn_bwd(info, mine, got, out_keep, out_send, grad_keep, grad_send, lse, hd):
    cols, tok = mine.shape
    heads_k = cols // (4 * hd)
    width = tok // 2
    keep = pl.BlockSpec((width, 2 * hd), lambda h, i, info: (keep_block(i, info), h))
    send = pl.BlockSpec((width, 2 * hd), lambda h, i, info: (send_block(i, info), h))
    full = pl.BlockSpec((cols, tok), lambda h, i, info: (0, 0))
    return pl.pallas_call(
        functools.partial(attn_bwd_kernel, width, hd),
        grid_spec=pltpu.PrefetchScalarGridSpec(
            num_scalar_prefetch=1,
            grid=(heads_k, 4),
            in_specs=[
                ANY,
                ANY,
                keep,
                send,
                keep,
                send,
                pl.BlockSpec((1, 2, width), lambda h, i, info: (h, 0, i)),
            ],
            out_specs=[full, full],
            scratch_shapes=[
                pltpu.VMEM((cols, 2 * tok), BF16),
                pltpu.VMEM((2 * tok, 2 * hd), BF16),
                pltpu.VMEM((2 * tok, hd), BF16),
                pltpu.VMEM((2 * tok, hd), F32),
                pltpu.VMEM((2 * tok, hd), F32),
                pltpu.SemaphoreType.DMA((2,)),
            ],
        ),
        out_shape=[shape_of((cols, tok), BF16), shape_of((cols, tok), BF16)],
        compiler_params=settings(2, 60),
        cost_estimate=cost(True, 26),
        name="attn_bwd",
    )(info, mine, got, out_keep, out_send, grad_keep, grad_send, lse)


def load_blocks(plan, pieces, target, sem):
    rows = target.shape[1] // 4

    @pl.when(pl.program_id(0) == 0)
    def _():
        for k, places in enumerate(plan):
            for p, (piece, row) in enumerate(places):
                src = pieces[piece].at[pl.ds(row, rows)]
                pltpu.make_async_copy(src, target.at[k, pl.ds(p * rows, rows)], sem).start()
        pltpu.make_async_copy(target, target, sem).wait()


def out_proj_kernel(plan, count, info, *refs):
    x_ref, a0, a1, b0, b1, gain_ref, r_ref, n_ref, nt_ref, att_ref, w_ref, sem = refs[count:]
    load_blocks(plan, refs, w_ref, sem)
    ctx = info[2]
    total = x_ref[...].astype(F32)
    for j, ref, side in ((0, a0, ctx), (1, a1, ctx), (0, b0, 1 - ctx), (1, b1, 1 - ctx)):
        block = 2 * side + j
        part = ref[...]
        att_ref[block] = part
        total = total + dot(part, w_ref[block], 1, 1)
    rho = lax.rsqrt(jnp.mean(total * total, axis=-1, keepdims=True) + EPS)
    normed = total * rho * gain_ref[...]
    r_ref[...] = total
    n_ref[...] = normed.astype(BF16)
    nt_ref[...] = normed.T.astype(BF16)


def out_proj(info, x, mine, theirs, weights, gain, tile):
    plan, pieces = weights
    tok, width = x.shape
    feats = pieces[0].shape[1]
    rows_of = lambda n: pl.BlockSpec((tile, n), lambda i, info: (i, 0))
    return pl.pallas_call(
        functools.partial(out_proj_kernel, plan, len(pieces)),
        grid_spec=pltpu.PrefetchScalarGridSpec(
            num_scalar_prefetch=1,
            grid=(tok // tile,),
            in_specs=[ANY] * len(pieces)
            + [rows_of(width)]
            + [rows_of(feats)] * 4
            + [pl.BlockSpec((1, width), lambda i, info: (0, 0))],
            out_specs=[
                rows_of(width),
                rows_of(width),
                pl.BlockSpec((width, tile), lambda i, info: (0, i)),
                pl.BlockSpec((4, tile, feats), lambda i, info: (0, i, 0)),
            ],
            scratch_shapes=[pltpu.VMEM((4, width, feats), BF16), pltpu.SemaphoreType.DMA],
        ),
        out_shape=[
            shape_of((tok, width), F32),
            shape_of((tok, width), BF16),
            shape_of((width, tok), BF16),
            shape_of((4, tok, feats), BF16),
        ],
        compiler_params=settings(1, 60),
        cost_estimate=cost(True),
        name="out_proj",
    )(info, *pieces, x, *mine, *theirs, gain)


def norm_two_back_kernel(plan, count, info, *refs):
    g_ref, r_ref, gr_ref, gain_ref, gres_ref, gat_ref, a0, a1, b0, b1, gg_ref, w_ref, sem = refs[count:]
    load_blocks(plan, refs, w_ref, sem)
    ctx = info[2]
    grad, resid = g_ref[...], r_ref[...]
    rho = lax.rsqrt(jnp.mean(resid * resid, axis=-1, keepdims=True) + EPS)
    unit = resid * rho
    scaled = grad * gain_ref[...]
    back = rho * (scaled - unit * jnp.mean(scaled * unit, axis=-1, keepdims=True))
    total = gr_ref[...] + back
    gres_ref[...] = total
    low = total.astype(BF16)
    gat_ref[...] = total.T.astype(BF16)

    @pl.when(pl.program_id(0) == 0)
    def _():
        gg_ref[...] = jnp.zeros_like(gg_ref)

    gg_ref[...] += jnp.sum(grad * unit, axis=0, keepdims=True)
    for j, ref, side in ((0, a0, ctx), (1, a1, ctx), (0, b0, 1 - ctx), (1, b1, 1 - ctx)):
        ref[...] = dot(low, w_ref[2 * side + j], 1, 0).astype(BF16)


def norm_two_back(info, grad, resid, grad_result, gain, weights, tile):
    plan, pieces = weights
    tok, width = grad.shape
    feats = pieces[0].shape[1]
    rows_of = lambda n: pl.BlockSpec((tile, n), lambda i, info: (i, 0))
    row = pl.BlockSpec((1, width), lambda i, info: (0, 0))
    return pl.pallas_call(
        functools.partial(norm_two_back_kernel, plan, len(pieces)),
        grid_spec=pltpu.PrefetchScalarGridSpec(
            num_scalar_prefetch=1,
            grid=(tok // tile,),
            in_specs=[ANY] * len(pieces) + [rows_of(width)] * 3 + [row],
            out_specs=[rows_of(width), pl.BlockSpec((width, tile), lambda i, info: (0, i))]
            + [rows_of(feats)] * 4
            + [row],
            scratch_shapes=[pltpu.VMEM((4, width, feats), BF16), pltpu.SemaphoreType.DMA],
        ),
        out_shape=[shape_of((tok, width), F32), shape_of((width, tok), BF16)]
        + [shape_of((tok, feats), BF16)] * 4
        + [shape_of((1, width), F32)],
        compiler_params=settings(1, 60),
        cost_estimate=cost(True, 9),
        name="norm_two_back",
    )(info, *pieces, grad, resid, grad_result, gain)


def norm_one_back_kernel(plan, count, info, *refs):
    p0, p1, x_ref, gres_ref, gain_ref, out_ref, gg_ref, w_ref, sem = refs[count:]
    load_blocks(plan, refs, w_ref, sem)
    quarter = x_ref.shape[1] // 4
    grad = dot(p0[0], w_ref[0], 1, 1)
    grad = grad + dot(p1[0], w_ref[1], 1, 1)
    grad = grad + dot(p0[1], w_ref[2], 1, 1)
    grad = grad + dot(p1[1], w_ref[3], 1, 1)
    x = x_ref[...].astype(F32)
    rho = lax.rsqrt(jnp.mean(x * x, axis=-1, keepdims=True) + EPS)
    unit = x * rho
    scaled = grad * gain_ref[...]
    back = rho * (scaled - unit * jnp.mean(scaled * unit, axis=-1, keepdims=True))
    total = (gres_ref[...] + back).astype(BF16)
    for p, mask in enumerate(MASKS):
        at = pl.multiple_of(jnp.bitwise_xor(info[1], mask) * quarter, quarter)
        part = total[:, p * quarter : (p + 1) * quarter]

        out_ref[:, pl.ds(at, quarter)] = part

    @pl.when(pl.program_id(0) == 0)
    def _():
        gg_ref[...] = jnp.zeros_like(gg_ref)

    gg_ref[...] += jnp.sum(grad * unit, axis=0, keepdims=True)


def norm_one_back(info, pairs, weights, x, grad_resid, gain, tile):
    plan, pieces = weights
    tok, width = x.shape
    cols = pieces[0].shape[1]
    rows_of = lambda n: pl.BlockSpec((tile, n), lambda i, info: (i, 0))
    pair = pl.BlockSpec((2, tile, cols), lambda i, info: (0, i, 0))
    row = pl.BlockSpec((1, width), lambda i, info: (0, 0))
    return pl.pallas_call(
        functools.partial(norm_one_back_kernel, plan, len(pieces)),
        grid_spec=pltpu.PrefetchScalarGridSpec(
            num_scalar_prefetch=1,
            grid=(tok // tile,),
            in_specs=[ANY] * len(pieces) + [pair, pair, rows_of(width), rows_of(width), row],
            out_specs=[rows_of(width), row],
            scratch_shapes=[pltpu.VMEM((4, width, cols), BF16), pltpu.SemaphoreType.DMA],
        ),
        out_shape=[shape_of((tok, width), BF16), shape_of((1, width), F32)],
        compiler_params=settings(1, 60),
        cost_estimate=cost(True),
        name="norm_one_back",
    )(info, *pieces, *pairs, x, grad_resid, gain)


def weight_copies(plan, pieces, gate_up, down, gate_up_sem, down_sem):
    third = down.shape[1] // 3
    rows = down.shape[0] // 4
    wide, thin = [], []
    for p, chunks in enumerate(plan):
        block = pl.ds(p * rows, rows)
        for j, (piece, row, at) in enumerate(chunks):
            src = pieces[piece].at[pl.ds(row, rows)]
            wide.append(
                pltpu.make_async_copy(
                    src.at[:, pl.ds(at, 2 * third)],
                    gate_up.at[block, pl.ds(j * 2 * third, 2 * third)],
                    gate_up_sem,
                )
            )
            thin.append(
                pltpu.make_async_copy(
                    src.at[:, pl.ds(at + 2 * third, third)],
                    down.at[block, pl.ds(j * third, third)],
                    down_sem,
                )
            )
    return wide, thin


def split_act(act):
    third = act.shape[1] // 6
    part = lambda j: act[:, j * third : (j + 1) * third]
    return [(part(0), part(1)), (part(2), part(3)), (part(4), part(5))]


def ffn_fwd_kernel(tile, plans, last, info, scale, x_ref, in_ref, *rest):
    if last:
        teach_ref, rest = rest[0], rest[1:]
    pieces = []
    for plan in plans:
        count = 1 + max(place[0] for chunks in plan for place in chunks)
        pieces.append(rest[:count])
        rest = rest[count:]
    act_ref, hid_ref = rest[:2]
    if last:
        out_ref, gres_ref, low_ref, lowt_ref, sq_ref = rest[2:7]
        gate_up, down, total, sems = rest[7:]
    else:
        sum_ref, gate_up, down, total, sems = rest[2:]
    step, part = pl.program_id(0), pl.program_id(1)
    final = len(plans) - 1
    width = x_ref.shape[1]
    quarter = width // 4
    third = down.shape[2] // 3

    def copies(s):
        return weight_copies(
            plans[s], pieces[s], gate_up.at[s], down.at[s], sems.at[s, 0], sems.at[s, 1]
        )

    @pl.when((step == 0) & (part == 0))
    def _():
        for s in range(len(plans)):
            wide, thin = copies(s)
            for copy in wide + thin:
                copy.start()

    for s in range(len(plans)):

        @pl.when((step == s) & (part == 0))
        def _():
            pltpu.make_async_copy(gate_up.at[s], gate_up.at[s], sems.at[s, 0]).wait()

    rows = pl.ds(pl.multiple_of(part * tile, tile), tile)
    act = dot(x_ref[rows, :], gate_up[step], 1, 0)
    for j, (gate, upper) in enumerate(split_act(act)):
        sig = sigmoid(gate)
        silu = gate * sig
        hid_ref[0, :, j * third : (j + 1) * third] = (silu * upper).astype(BF16)
        at = 2 * j * third
        act_ref[0, :, at : at + third] = (upper * (sig + silu - silu * sig)).astype(BF16)
        act_ref[0, :, at + third : at + 2 * third] = silu.astype(BF16)
    for s in range(len(plans)):

        @pl.when((step == s) & (part == 0))
        def _():
            pltpu.make_async_copy(down.at[s], down.at[s], sems.at[s, 1]).wait()

    grown = dot(hid_ref[0], down[step], 1, 1)

    @pl.when(step == 0)
    def _():
        total[rows, :] = in_ref[...] + grown

    @pl.when(step > 0)
    def _():
        total[rows, :] += grown

    @pl.when(step == final)
    def _():
        result = total[rows, :]
        if not last:
            sum_ref[...] = result
            return
        tok = x_ref.shape[0]
        slot = info[2] * tok + part * tile + lax.broadcasted_iota(jnp.int32, (tile, 1), 0)
        valid = jnp.where(slot < info[3], 1.0, 0.0)
        square = jnp.zeros((tile, quarter), F32)
        for p, mask in enumerate(MASKS):
            at = pl.multiple_of(jnp.bitwise_xor(info[1], mask) * quarter, quarter)
            cols = slice(p * quarter, (p + 1) * quarter)
            value = result[:, cols]
            out_ref[:, pl.ds(at, quarter)] = value.astype(BF16)
            error = valid * (value - teach_ref[0, :, pl.ds(at, quarter)].astype(F32))
            square = square + error * error
            grad = error * scale[0]
            gres_ref[:, cols] = grad
            low_ref[:, cols] = grad.astype(BF16)
            lowt_ref[cols, :] = grad.T.astype(BF16)

        @pl.when(part == 0)
        def _():
            sq_ref[...] = jnp.zeros_like(sq_ref)

        sq_ref[...] += jnp.sum(square, axis=0, keepdims=True)


def ffn_fwd(info, scale, x, total, teacher, weights, units, tile):
    tok, width = x.shape
    pieces = [piece for _, group in weights for piece in group]
    count = len(weights)
    last = teacher is not None
    entry = lambda s, i: jnp.where(s == 0, i, tok // tile - 1)
    leave = lambda s, i: jnp.where(s == count - 1, i, 0)
    tiles = lambda n: pl.BlockSpec((tile, n), lambda s, i, info: (leave(s, i), 0))
    slab = lambda n: pl.BlockSpec((1, tile, n), lambda s, i, info: (s, i, 0))
    in_specs = [
        SMEM,
        whole((tok, width)),
        pl.BlockSpec((tile, width), lambda s, i, info: (entry(s, i), 0)),
    ]
    out_specs = [slab(2 * units), slab(units)]
    out_shape = [shape_of((count, tok, 2 * units), BF16), shape_of((count, tok, units), BF16)]
    if last:
        in_specs.append(
            pl.BlockSpec((1, tile, width), lambda s, i, info: (info[0], leave(s, i), 0))
        )
        out_specs += [
            tiles(width),
            tiles(width),
            tiles(width),
            pl.BlockSpec((width, tile), lambda s, i, info: (0, leave(s, i))),
            pl.BlockSpec((1, width // 4), lambda s, i, info: (0, 0)),
        ]
        out_shape += [
            shape_of((tok, width), BF16),
            shape_of((tok, width), F32),
            shape_of((tok, width), BF16),
            shape_of((width, tok), BF16),
            shape_of((1, width // 4), F32),
        ]
    else:
        out_specs.append(tiles(width))
        out_shape.append(shape_of((tok, width), F32))
    return pl.pallas_call(
        functools.partial(ffn_fwd_kernel, tile, [plan for plan, _ in weights], last),
        grid_spec=pltpu.PrefetchScalarGridSpec(
            num_scalar_prefetch=1,
            grid=(count, tok // tile),
            in_specs=in_specs + [ANY] * len(pieces),
            out_specs=out_specs,
            scratch_shapes=[
                pltpu.VMEM((count, width, 2 * units), BF16),
                pltpu.VMEM((count, width, units), BF16),
                pltpu.VMEM((tok, width), F32),
                pltpu.SemaphoreType.DMA((count, 2)),
            ],
        ),
        out_shape=out_shape,
        compiler_params=settings(2, 60),
        cost_estimate=cost(True),
        name="ffn_fwd",
    )(info, scale, x, total, *([teacher] if last else []), *pieces)


def ffn_bwd_kernel(steps, plan, first, low_ref, act_ref, hid_ref, xt_ref, lowt_ref, *rest):
    count = 1 + max(place[0] for chunks in plan for place in chunks)
    pieces, rest = rest[:count], rest[count:]
    if not first:
        in_ref, rest = rest[0], rest[1:]
    out_ref, keep_ref, send_ref, gate_up, down, dact_all, hid_all, sems = rest
    step = pl.program_id(0)
    units = down.shape[1]
    third = units // 3
    tile = low_ref.shape[0]

    @pl.when(step == 0)
    def _():
        wide, thin = weight_copies(plan, pieces, gate_up, down, sems.at[0], sems.at[1])
        for copy in thin + wide:
            copy.start()
        pltpu.make_async_copy(down, down, sems.at[1]).wait()

    @pl.when(step < steps)
    def _():
        rows = pl.ds(pl.multiple_of(step * tile, tile), tile)
        grad_hidden = dot(low_ref[...], down[...], 1, 0)
        for j, (to_gate, to_upper) in enumerate(split_act(act_ref[0])):
            grad = grad_hidden[:, j * third : (j + 1) * third]
            at = 2 * j * third
            dact_all[rows, at : at + third] = (grad * to_gate.astype(F32)).astype(BF16)
            dact_all[rows, at + third : at + 2 * third] = (grad * to_upper.astype(F32)).astype(BF16)
        hid_all[rows, :] = hid_ref[0]

        @pl.when(step == 0)
        def _():
            pltpu.make_async_copy(gate_up, gate_up, sems.at[0]).wait()

        grown = dot(dact_all[rows, :], gate_up[...], 1, 1)
        out_ref[...] = grown if first else in_ref[...] + grown

    def weight_rows(target):
        target[:, : 2 * units] = dot(xt_ref[...], dact_all[...], 1, 0).astype(BF16)
        target[:, 2 * units :] = dot(lowt_ref[...], hid_all[...], 1, 0).astype(BF16)

    @pl.when((step >= steps) & (step < steps + 2))
    def _():
        weight_rows(send_ref)

    @pl.when(step >= steps + 2)
    def _():
        weight_rows(keep_ref)


def ffn_bwd(low, saved, weights, total, xt, lowt, tile):
    plan, pieces = weights
    acts, hiddens, block = saved
    tok, width = low.shape
    units = hiddens.shape[2]
    steps = tok // tile
    quarter = width // 4
    first = total is None
    clip = lambda i: jnp.minimum(i, steps - 1)
    rows_of = lambda n: pl.BlockSpec((tile, n), lambda i: (clip(i), 0))
    slab = lambda n: pl.BlockSpec((1, tile, n), lambda i: (block, clip(i), 0))
    feature = lambda i: (jnp.where(i < steps + 2, jnp.maximum(i - steps, 0) + 2, i - steps - 2), 0)
    return pl.pallas_call(
        functools.partial(ffn_bwd_kernel, steps, plan, first),
        grid=(steps + 4,),
        in_specs=[
            rows_of(width),
            slab(2 * units),
            slab(units),
            pl.BlockSpec((quarter, tok), feature),
            pl.BlockSpec((quarter, tok), feature),
        ]
        + [ANY] * len(pieces)
        + ([] if first else [rows_of(width)]),
        out_specs=[
            rows_of(width),
            pl.BlockSpec((quarter, 3 * units), lambda i: (jnp.maximum(i - steps - 2, 0), 0)),
            pl.BlockSpec((quarter, 3 * units), lambda i: (jnp.clip(i - steps, 0, 1), 0)),
        ],
        out_shape=[
            shape_of((tok, width), F32),
            shape_of((width // 2, 3 * units), BF16),
            shape_of((width // 2, 3 * units), BF16),
        ],
        scratch_shapes=[
            pltpu.VMEM((width, 2 * units), BF16),
            pltpu.VMEM((width, units), BF16),
            pltpu.VMEM((tok, 2 * units), BF16),
            pltpu.VMEM((tok, units), BF16),
            pltpu.SemaphoreType.DMA((2,)),
        ],
        input_output_aliases={} if first else {5 + len(pieces): 0},
        compiler_params=settings(1, 60),
        cost_estimate=cost(True, 18),
        name="ffn_bwd",
    )(low, acts, hiddens, xt, lowt, *pieces, *([] if first else [total]))


def turn_chunks(block):
    wide = block.shape[1] * 2 // 9
    thin = wide // 2
    starts = [(2 * wide, wide), (wide, wide), (0, wide)]
    starts += [(3 * wide + 2 * thin, thin), (3 * wide + thin, thin), (3 * wide, thin)]
    return jnp.concatenate([block[:, a : a + n] for a, n in starts], axis=1)


def sum_kernel(turns, *refs):
    total = None
    for ref, turn in zip(refs[:-1], turns):
        value = ref[...].astype(F32)
        value = turn_chunks(value) if turn else value
        total = value if total is None else total + value
    refs[-1][...] = total.astype(refs[-1].dtype)


def summed(terms, turns=None, dtype=BF16):
    rows, cols = terms[0].shape
    spec = pl.BlockSpec((128, cols), lambda i: (i, 0))
    return pl.pallas_call(
        functools.partial(sum_kernel, turns or [False] * len(terms)),
        grid=(rows // 128,),
        in_specs=[spec] * len(terms),
        out_specs=spec,
        out_shape=shape_of((rows, cols), dtype),
        compiler_params=settings(1, 60),
        cost_estimate=cost(False),
        name="summed",
    )(*terms)


def sums_kernel(jobs, count, info, *refs):
    arrays, refs = refs[:count], refs[count:]
    outs, (term_buf, out_buf, term_sems, out_sems) = refs[: len(jobs)], refs[len(jobs) :]
    rows = term_buf.shape[1]
    copies = []
    for terms in jobs:
        group = []
        for array, base, pick, _ in terms:
            at = base
            if pick is not None:
                at = pl.multiple_of(base + jnp.bitwise_xor(info[2], pick) * rows, rows)
            i = len(copies) + len(group)
            src = arrays[array].at[pl.ds(at, rows)]
            group.append(pltpu.make_async_copy(src, term_buf.at[i], term_sems.at[i]))
            group[-1].start()
        copies += group
    first = 0
    stores = []
    for j, terms in enumerate(jobs):
        total = None
        for i, (_, _, _, turn) in enumerate(terms):
            copies[first + i].wait()
            value = term_buf[first + i].astype(F32)
            value = turn_chunks(value) if turn else value
            total = value if total is None else total + value
        first += len(terms)
        out_buf[j] = total.astype(BF16)
        stores.append(pltpu.make_async_copy(out_buf.at[j], outs[j], out_sems.at[j]))
        stores[-1].start()
    for store in stores:
        store.wait()


def sums(info, arrays, jobs):
    cols = arrays[0].shape[1]
    rows, terms = 128, sum(len(job) for job in jobs)
    return pl.pallas_call(
        functools.partial(sums_kernel, jobs, len(arrays)),
        grid_spec=pltpu.PrefetchScalarGridSpec(
            num_scalar_prefetch=1,
            grid=(1,),
            in_specs=[ANY] * len(arrays),
            out_specs=[ANY] * len(jobs),
            scratch_shapes=[
                pltpu.VMEM((terms, rows, cols), BF16),
                pltpu.VMEM((len(jobs), rows, cols), BF16),
                pltpu.SemaphoreType.DMA((terms,)),
                pltpu.SemaphoreType.DMA((len(jobs),)),
            ],
        ),
        out_shape=[shape_of((rows, cols), BF16)] * len(jobs),
        compiler_params=settings(1, 60),
        cost_estimate=cost(False),
        name="sums",
    )(info, *arrays)


def core_jobs(keep, came):
    return [[(a, far * 256, pick, False) for a in (keep, came)] for far in (0, 1) for pick in (0, 1)]


def core_sum_kernel(info, left_ref, right_ref, *outs):
    total = (left_ref[...].astype(F32) + right_ref[...].astype(F32)).astype(BF16)
    block = pl.program_id(1)
    place = block // 2 * 2 + jnp.bitwise_xor(block % 2, info[2])
    for i, out in enumerate(outs):

        @pl.when(place == i)
        def _():
            out[...] = total


def core_sum(info, keep, came):
    groups, rows, cols = keep.shape
    spec = pl.BlockSpec((1, rows // 4, cols), lambda g, i, info: (g, i, 0))
    return pl.pallas_call(
        core_sum_kernel,
        grid_spec=pltpu.PrefetchScalarGridSpec(
            num_scalar_prefetch=1,
            grid=(groups, 4),
            in_specs=[spec] * 2,
            out_specs=[pl.BlockSpec((1, rows // 4, cols), lambda g, i, info: (g, 0, 0))] * 4,
        ),
        out_shape=[shape_of((groups, rows // 4, cols), BF16)] * 4,
        compiler_params=settings(2, 24),
        cost_estimate=cost(False),
        name="core_sum",
    )(info, keep, came)


def weight_grad_kernel(nt_ref, back0_ref, back1_ref, gt_ref, att_ref, keep_ref, send_ref):
    cols = back0_ref.shape[2]
    part, block = pl.program_id(0), pl.program_id(1)

    def rows(target, back_ref):
        target[0, :, :cols] = dot(nt_ref[...], back_ref[0], 1, 0).astype(BF16)
        target[0, :, cols:] = dot(gt_ref[...], att_ref[0], 1, 0).astype(BF16)

    for j, back_ref in enumerate((back0_ref, back1_ref)):

        @pl.when((part == 0) & (block % 2 == j))
        def _():
            rows(send_ref, back_ref)

        @pl.when((part == 1) & (block % 2 == j))
        def _():
            rows(keep_ref, back_ref)


def weight_grad(normed_t, backs, grad_t, attended):
    width, tok = normed_t.shape
    cols, feats = backs[0].shape[2], attended.shape[2]
    half = pl.BlockSpec((width // 2, tok), lambda p, k: (1 - p, 0))
    side = pl.BlockSpec((1, tok, cols), lambda p, k: (k // 2, 0, 0))
    shape = (1, width // 2, cols + feats)
    return pl.pallas_call(
        weight_grad_kernel,
        grid=(2, 4),
        in_specs=[half, side, side, half, pl.BlockSpec((1, tok, feats), lambda p, k: (k, 0, 0))],
        out_specs=[
            pl.BlockSpec(shape, lambda p, k: (jnp.where(p == 0, 0, k), 0, 0)),
            pl.BlockSpec(shape, lambda p, k: (jnp.where(p == 0, k, 3), 0, 0)),
        ],
        out_shape=[shape_of((4, width // 2, cols + feats), BF16)] * 2,
        compiler_params=settings(2, 60),
        cost_estimate=cost(True),
        name="weight_grad",
    )(normed_t, *backs, grad_t, attended)


def after(value, *others):
    return lax.optimization_barrier((value,) + others)[0]


def per_device_rows(
    tokens,
    teacher,
    lengths,
    attn_gain,
    q_weight,
    k_weight,
    v_weight,
    q_gain,
    k_gain,
    o_weight,
    ffn_gain,
    gate_weight,
    up_weight,
    down_weight,
):
    z = lax.axis_index("tp")
    ctx = lax.axis_index("ctx")
    fsdp = lax.axis_index("fsdp")
    rows_dev, tok, width = tokens.shape
    quarter = width // 4
    hd = q_gain.shape[0] * 4
    q_cols, k_cols = q_weight.shape[1], k_weight.shape[1]
    proj = q_cols + 2 * k_cols
    heads = (q_cols // hd, k_cols // hd)
    units = gate_weight.shape[1]
    slots = rows_dev * 4 * tok * 2

    def x_swap(v):
        return lax.ppermute(v, "fsdp", X_SWAP)

    def core_swap(v):
        return lax.ppermute(v, "fsdp", CORE_SWAP)

    def y_swap(v):
        return lax.ppermute(v, "ctx", Y_SWAP)

    def z_up(v):
        return lax.ppermute(v, "tp", Z_UP)

    def z_far(v):
        return lax.ppermute(v, "tp", Z_FAR)

    def z_down(v):
        return lax.ppermute(v, "tp", Z_DOWN)

    def natural(v):
        v = jnp.concatenate([v[0:1], v[2:3], v[1:2], v[3:4]], axis=0)
        v = jnp.where(fsdp % 2 == 0, v, jnp.concatenate([v[1:2], v[0:1], v[3:4], v[2:3]], axis=0))
        return jnp.where(fsdp // 2 == 0, v, jnp.concatenate([v[2:4], v[0:2]], axis=0))

    v = {}

    def sync():
        v.update(lax.optimization_barrier(dict(v)))

    length = lax.dynamic_slice_in_dim(lengths, z, 1, 0)
    info = jnp.concatenate([jnp.stack([z, fsdp, ctx]).astype(jnp.int32), length])
    w_proj = join(q_weight, k_weight, v_weight)
    proj_z = [z_up(w_proj), z_far(w_proj), z_down(w_proj)]
    proj_own = jnp.concatenate([w_proj, x_swap(w_proj)], axis=0)
    count_here = jnp.sum(lengths).astype(F32)[None]
    vector = jnp.concatenate([attn_gain, ffn_gain, q_gain, k_gain]).astype(F32)
    vector = jnp.concatenate([vector, count_here, jnp.zeros((640 - 545,), F32)])[None]
    vector = jnp.concatenate([vector, x_swap(vector)], axis=0)
    vector = jnp.concatenate([vector, core_swap(vector)], axis=0)
    w_out, w_ffn, *w_chunks = pack(info, o_weight, gate_weight, up_weight, down_weight)
    pos = (ctx * tok + jnp.arange(tok, dtype=jnp.int32)).astype(F32)
    frequency = THETA ** (-(2.0 * jnp.arange(hd // 2, dtype=F32)) / hd)
    angles = frequency[:, None] * pos[None, :]
    head_gains = natural(vector[:, 2 * quarter : 544])
    v.update(
        info=info,
        proj_own=proj_own,
        proj_z=jnp.concatenate(proj_z, axis=0),
        w_out=w_out,
        w_ffn=w_ffn,
        w_chunks=w_chunks,
        gain_one=vector[:, :quarter].reshape(1, width),
        gain_two=vector[:, quarter : 2 * quarter].reshape(1, width),
        total_count=jnp.sum(vector[:, 544]),
        gain_q=head_gains[:, : hd // 4].reshape(hd, 1),
        gain_k=head_gains[:, hd // 4 :].reshape(hd, 1),
        cos_part=jnp.cos(angles),
        sin_part=jnp.sin(angles),
    )
    sync()
    info = v["info"]

    proj_zfar = x_swap(v["proj_z"])
    out_z = [z_up(v["w_out"]), z_far(v["w_out"]), z_down(v["w_out"])]
    own_core = core_swap(v["proj_own"])
    x_in, normed_one_t = norm_one(info, tokens, v["gain_one"], 256)
    v.update(
        proj_zfar=proj_zfar, own_core=own_core, x_in=x_in, normed_one_t=normed_one_t, out_z=out_z
    )
    sync()

    plan_proj = [[(0, 0), (0, quarter), (3, 0), (3, quarter)]]
    plan_proj += [[(p, k * quarter) for p in (1, 2, 4, 5)] for k in range(3)]
    weights_proj = [v["proj_own"], v["proj_z"], v["proj_zfar"], v["own_core"]]
    weights_proj += [core_swap(v["proj_z"]), core_swap(v["proj_zfar"])]
    one = [z_up(v["w_chunks"][0]), z_up(v["w_chunks"][3])]
    ffn_far = x_swap(v["w_ffn"])
    tables = [v[name] for name in ("cos_part", "sin_part", "gain_q", "gain_k")]

    def make(block, *then):
        normed_t = after(v["normed_one_t"], *then)
        return project(info, (plan_proj, weights_proj), normed_t, *tables, heads, block)

    theirs = [make(lambda s: 2 * (1 - s[2]))]
    got = [y_swap(theirs[0][0])]
    theirs.append(make(lambda s: 2 * (1 - s[2]) + 1, theirs[0][0]))
    got.append(y_swap(theirs[1][0]))
    mine = [make(lambda s: 2 * s[2], theirs[1][0])]
    mine.append(make(lambda s: 2 * s[2] + 1, mine[0][0]))
    v.update(
        one=one,
        ffn_far=ffn_far,
        weights_proj=weights_proj,
        mine=mine,
        theirs=theirs,
        got0=got[0],
    )
    sync()

    one_far = [x_swap(v["one"][0])]
    three = [z_down(v["w_chunks"][0])]
    own_cores = [core_swap(v["w_ffn"]), core_swap(v["ffn_far"])]
    first = attn_fwd(info, v["mine"][0][0], v["got0"], hd)
    v.update(first=first, got1=got[1], one_far=one_far, three=three, own_cores=own_cores)
    sync()

    arrived = [y_swap(v["first"][1])]
    three = v["three"] + [z_down(v["w_chunks"][1])]
    out_blocks = jnp.concatenate([v["w_out"]] + v["out_z"], axis=0)
    out_far = x_swap(out_blocks)
    one_cores = [core_swap(v["one"][0]), core_swap(v["one_far"][0])]
    second = attn_fwd(info, v["mine"][1][0], v["got1"], hd)
    v.update(
        second=second,
        arrived=arrived,
        three=three,
        out_blocks=out_blocks,
        out_far=out_far,
        one_cores=one_cores,
    )
    sync()

    arrived = v["arrived"] + [y_swap(v["second"][1])]
    three = v["three"] + [z_down(v["w_chunks"][2])]
    one_far = v["one_far"] + [x_swap(v["one"][1][:, :units])]
    weights_out = [v["out_blocks"], v["out_far"]]
    weights_out += [core_swap(v["out_blocks"]), core_swap(v["out_far"])]
    v.update(arrived=arrived, three=three, one_far=one_far, weights_out=weights_out)
    sync()

    plan_out = [[(p, k * quarter) for p in range(4)] for k in range(4)]
    two = [z_up(v["one"][0])]
    three_far = [x_swap(v["three"][0])]
    one_far = v["one_far"] + [y_swap(v["one_far"][0])]
    one_cores = v["one_cores"] + [core_swap(v["one"][1]), core_swap(v["one_far"][1])]
    resid, normed_two, normed_two_t, attended = out_proj(
        info,
        v["x_in"],
        [v["first"][0], v["second"][0]],
        v["arrived"],
        (plan_out, v["weights_out"]),
        v["gain_two"],
        256,
    )
    v.update(
        two=two,
        three_far=three_far,
        one_far=one_far,
        one_cores=one_cores,
        resid=resid,
        normed_two=normed_two,
        normed_two_t=normed_two_t,
        attended=attended,
    )
    sync()

    plan0 = [[(i, 0, j * units) for j in range(3)] for i in range(4)]
    plan_mixed = [[(0, 0, 0), (1, 0, 0), (1, 0, units)], [(i, 0, 0) for i in (2, 3, 4)]]
    plan_mixed += [[(5, 0, 0), (6, 0, 0), (6, 0, units)], [(i, 0, 0) for i in (7, 8, 9)]]
    scale = (slots / v["total_count"])[None]
    weights0 = [v["w_ffn"], v["ffn_far"]] + v["own_cores"]
    c0, cf, c1, cb = v["one_cores"]
    weights1 = v["one"] + v["one_far"] + [c0, c1, cf, cb, core_swap(v["one_far"][2])]
    two = v["two"] + [z_up(v["one"][1])]
    three_far = v["three_far"] + [x_swap(v["three"][1]), y_swap(v["three_far"][0])]
    two_far = [x_swap(v["two"][0])]
    three_cores = [core_swap(v["three"][0])]
    acts_a, hiddens_a, sum_a = ffn_fwd(
        info,
        scale,
        v["normed_two"],
        v["resid"],
        None,
        [(plan0, weights0), (plan_mixed, weights1)],
        units,
        256,
    )
    v.update(
        scale=scale,
        weights0=weights0,
        weights1=weights1,
        two=two,
        three_far=three_far,
        two_far=two_far,
        three_cores=three_cores,
        acts_a=acts_a,
        hiddens_a=hiddens_a,
        sum_a=sum_a,
    )
    sync()

    plan_chunks = [[(3 * p + j, 0, 0) for j in range(3)] for p in range(4)]
    weights3 = v["three"] + v["three_far"] + v["three_cores"]
    weights3 += [core_swap(part) for part in v["three"][1:]]
    weights3 += [core_swap(part) for part in v["three_far"]]
    two_far = v["two_far"] + [x_swap(v["two"][1][:, :units]), y_swap(v["two_far"][0])]
    two_cores = [core_swap(part) for part in v["two"] + v["two_far"]]
    acts_b, hiddens_b, sum_b = ffn_fwd(
        info, v["scale"], v["normed_two"], v["sum_a"], None, [(plan_chunks, weights3)], units, 256
    )
    v.update(
        weights3=weights3,
        two_far=two_far,
        two_cores=two_cores,
        acts_b=acts_b,
        hiddens_b=hiddens_b,
        sum_b=sum_b,
    )
    sync()

    weights2 = v["two"] + v["two_far"] + v["two_cores"]
    weights2 += [core_swap(part) for part in v["two_far"][1:]]
    acts_c, hiddens_c, result_low, grad_result, grad_low, grad_low_t, square = ffn_fwd(
        info, v["scale"], v["normed_two"], v["sum_b"], teacher, [(plan_mixed, weights2)], units, 256
    )
    v.update(
        weights2=weights2,
        acts_c=acts_c,
        hiddens_c=hiddens_c,
        result_low=result_low,
        grad_result=grad_result,
        grad_low=grad_low,
        grad_low_t=grad_low_t,
        square=square,
    )
    sync()

    def ffn_back(plan, weights, acts, hiddens, block, total):
        return ffn_bwd(
            v["grad_low"],
            (v[acts], v[hiddens], block),
            (plan, v[weights]),
            total,
            v["normed_two_t"],
            v["grad_low_t"],
            256,
        )

    turned = [False, False, True]
    output = lax.all_gather(v["result_low"], "tp", axis=0, tiled=False)
    total, keep2, send2 = ffn_back(plan_mixed, "weights2", "acts_c", "hiddens_c", 0, None)
    v.update(total=total, keep2=keep2, send2=send2)
    sync()

    came2 = core_swap(v["send2"])
    total, keep1, send1 = ffn_back(plan_mixed, "weights1", "acts_a", "hiddens_a", 1, v["total"])
    v.update(came2=came2, total=total, keep1=keep1, send1=send1)
    sync()

    came1 = core_swap(v["send1"])
    sum2 = sums(info, [v["keep2"], v["came2"]], core_jobs(0, 1))
    far_t2 = x_swap(sum2[3])
    total, keep3, send3 = ffn_back(
        plan_chunks, "weights3", "acts_b", "hiddens_b", 0, after(v["total"], sum2[0])
    )
    v.update(
        came1=came1,
        sum2=sum2,
        far_t2=far_t2,
        total=total,
        keep3=keep3,
        send3=send3,
    )
    sync()

    came3 = core_swap(v["send3"])
    far_h2 = x_swap(v["sum2"][2])
    there2, *sum1 = sums(
        info,
        [v["sum2"][1], v["far_t2"], v["keep1"], v["came1"]],
        [[(0, 0, None, False), (1, 0, None, False)]] + core_jobs(2, 3),
    )
    there2 = y_swap(there2)
    total, keep0, send0 = ffn_back(
        plan0, "weights0", "acts_a", "hiddens_a", 0, after(v["total"], sum1[0])
    )
    v.update(
        came3=came3,
        far_h2=far_h2,
        there2=there2,
        sum1=sum1,
        total=total,
        keep0=keep0,
        send0=send0,
    )
    sync()

    came0 = core_swap(v["send0"])
    far_t1 = x_swap(v["sum1"][3])
    plane = [(0, 0, None, False), (1, 0, None, False), (2, 0, None, True)]
    part2, *sum3 = sums(
        info,
        [v["sum2"][0], v["far_h2"], v["there2"], v["keep3"], v["came3"]],
        [plane] + core_jobs(3, 4),
    )
    down2 = z_down(part2)
    grad_resid, grad_attn_t, a0, a1, b0, b1, gain_two_sum = norm_two_back(
        info,
        after(v["total"], sum3[0]),
        v["resid"],
        v["grad_result"],
        v["gain_two"],
        (plan_out, v["weights_out"]),
        256,
    )
    grad_got = [y_swap(b0), y_swap(b1)]
    v.update(
        came0=came0,
        far_t1=far_t1,
        down2=down2,
        sum3=sum3,
        grad_resid=grad_resid,
        grad_attn_t=grad_attn_t,
        grad_mine=[a0, a1],
        gain_two_sum=gain_two_sum,
        grad_got0=grad_got[0],
    )
    sync()

    def attn_back(j, grad):
        out, got_ref = v["first" if j == 0 else "second"], v[f"got{j}"]
        return attn_bwd(
            info, v["mine"][j][0], got_ref, out[0], out[1], grad, v[f"grad_got{j}"], out[2], hd
        )

    far_h1 = x_swap(v["sum1"][2])
    [there1] = sums(
        info, [v["sum1"][1], v["far_t1"]], [[(0, 0, None, False), (1, 0, None, False)]]
    )
    there1_got = y_swap(there1)
    far_t3 = x_swap(v["sum3"][3])
    back0 = attn_back(0, after(v["grad_mine"][0], there1))
    v.update(
        far_h1=far_h1,
        there1=there1_got,
        far_t3=far_t3,
        output=output,
        back0=back0,
        grad_got1=grad_got[1],
    )
    sync()

    heads0 = y_swap(v["back0"][1])
    far_h3 = x_swap(v["sum3"][2])
    there3, two_down = sums(
        info,
        [v["sum3"][1], v["far_t3"], v["sum1"][0], v["far_h1"], v["there1"], v["down2"]],
        [
            [(0, 0, None, False), (1, 0, None, False)],
            [(2, 0, None, False), (3, 0, None, False), (4, 0, None, True), (5, 0, None, False)],
        ],
    )
    there3_got = y_swap(there3)
    two_down_got = z_down(two_down)
    back1 = attn_back(1, after(v["grad_mine"][1], there3, two_down))
    v.update(
        heads0=heads0, far_h3=far_h3, there3=there3_got, back1=back1
    )
    sync()

    heads1 = y_swap(v["back1"][1])
    [part3] = sums(info, [v["sum3"][0], v["far_h3"], v["there3"]], [plane])
    up3 = z_up(part3)
    tables = [v[name] for name in ("cos_part", "sin_part", "gain_q", "gain_k")]
    head0 = head_back(
        info, v["back0"][0], v["heads0"], v["mine"][0][1], v["theirs"][0][1], *tables, heads
    )
    v.update(heads1=heads1, two_down=two_down_got, head0=head0)
    sync()

    head1 = head_back(
        info, v["back1"][0], v["heads1"], v["mine"][1][1], v["theirs"][1][1], *tables, heads
    )
    tokens_low, gain_one_sum = norm_one_back(
        info,
        [v["head0"][0], head1[0]],
        (plan_proj, v["weights_proj"]),
        v["x_in"],
        v["grad_resid"],
        v["gain_one"],
        tok // 4,
    )
    v.update(head1=head1, tokens_low=tokens_low, gain_one_sum=gain_one_sum, up3=up3)
    sync()

    gathered = lax.all_gather(v["tokens_low"], "tp", axis=0, tiled=False)
    keep, send = weight_grad(
        v["normed_one_t"], [v["head0"][0], v["head1"][0]], v["grad_attn_t"], v["attended"]
    )
    gain_heads = v["head0"][1] + v["head1"][1]
    vector = jnp.concatenate(
        [
            natural(v["gain_one_sum"].reshape(4, quarter)).reshape(1, width),
            natural(v["gain_two_sum"].reshape(4, quarter)).reshape(1, width),
            gain_heads[:, 0].reshape(1, hd),
            gain_heads[:, 1].reshape(1, hd),
            jnp.sum(v["square"]).reshape(1, 1),
            jnp.zeros((1, 127), F32),
        ],
        axis=1,
    )
    vector = vector + core_swap(vector)
    v.update(keep=keep, send=send)
    v.update(vector=vector)
    sync()

    rows = quarter // 2
    flat = lambda a: a.reshape(4 * rows, a.shape[-1])
    attn_sums = [flat(p) for p in core_sum(info, v["keep"], core_swap(v["send"]))]
    vector = v["vector"] + x_swap(v["vector"])
    sum0 = sums(info, [v["keep0"], v["came0"]], core_jobs(0, 1))
    v.update(sums=attn_sums, vector=vector, sum0=sum0)
    sync()

    far_t = x_swap(v["sums"][3])
    far_t0 = x_swap(v["sum0"][3])
    vector = v["vector"] + y_swap(v["vector"])
    v.update(far_t=far_t, far_t0=far_t0, vector=vector)
    sync()

    far_h = x_swap(v["sums"][2])
    there = y_swap(summed([v["sums"][1], v["far_t"]]))
    far_h0 = x_swap(v["sum0"][2])
    there0 = y_swap(summed([v["sum0"][1], v["far_t0"]]))
    v.update(far_h=far_h, there=there, far_h0=far_h0, there0=there0)
    sync()

    parts = summed([v["sums"][0], v["far_h"], v["there"]])
    parts = [parts[k * rows : (k + 1) * rows] for k in range(4)]
    parts = [parts[0], z_down(parts[1]), z_far(parts[2]), z_up(parts[3])]
    part0 = summed([v["sum0"][0], v["far_h0"], v["there0"]], turned)
    ffn_sum = summed([part0, v["two_down"], v["up3"]], None, F32)
    ffn_other = y_swap(ffn_sum)
    v.update(parts=parts, ffn_sum=ffn_sum)
    sync()

    attn_sum = summed(v["parts"], None, F32)
    vector = v["vector"] + lax.ppermute(v["vector"], "tp", Z_NEAR)
    v.update(attn_sum=attn_sum, vector=vector)
    v.update(ffn_other=ffn_other)
    sync()

    def finish(own, other):
        return jnp.concatenate(
            [jnp.where(ctx == 0, own, other), jnp.where(ctx == 0, other, own)], axis=0
        )

    def columns(first):
        parts = [ffn_grad[:, first(j) : first(j) + third] for j in range(3)]
        return jnp.concatenate(
            [
                jnp.where(ctx == 0, parts[0], parts[2]),
                parts[1],
                jnp.where(ctx == 0, parts[2], parts[0]),
            ],
            axis=1,
        )

    attn_other = y_swap(v["attn_sum"])
    vector = v["vector"] + lax.ppermute(v["vector"], "tp", Z_FAR)
    third = units // 3
    ffn_grad = finish(v["ffn_sum"], turn_chunks(v["ffn_other"]))
    grad_gate = columns(lambda j: 2 * j * third)
    grad_up = columns(lambda j: (2 * j + 1) * third)
    grad_down = columns(lambda j: 2 * units + j * third).T
    v.update(vector=vector, attn_other=attn_other)
    v.update(grad_gate=grad_gate, grad_up=grad_up, grad_down=grad_down)
    sync()

    tokens_grad = gathered.astype(F32)
    sums_all = v["vector"][0]

    attn_grad = finish(v["attn_sum"], v["attn_other"])
    teacher_loss = sums_all[2 * width + 2 * hd] / (v["total_count"] * width)

    def own_part(at, size):
        return lax.dynamic_slice_in_dim(sums_all, at + fsdp * (size // 4), size // 4, 0)

    return (
        v["output"],
        teacher_loss,
        tokens_grad,
        own_part(0, width),
        attn_grad[:, :q_cols],
        attn_grad[:, q_cols : q_cols + k_cols],
        attn_grad[:, q_cols + k_cols : proj],
        own_part(2 * width, hd),
        own_part(2 * width + hd, hd),
        attn_grad[:, proj:].T,
        own_part(width, width),
        v["grad_gate"],
        v["grad_up"],
        v["grad_down"],
    )


def solution(mesh):
    return jax.shard_map(
        per_device_rows if fits(mesh) else per_device_any,
        mesh=mesh,
        in_specs=(
            P("fsdp", "ctx", None),
            P("fsdp", "ctx", None),
            P("fsdp"),
            P("fsdp"),
            P("fsdp", "tp"),
            P("fsdp", "tp"),
            P("fsdp", "tp"),
            P("fsdp"),
            P("fsdp"),
            P("tp", "fsdp"),
            P("fsdp"),
            P("fsdp", "tp"),
            P("fsdp", "tp"),
            P("tp", "fsdp"),
        ),
        out_specs=(
            P("fsdp", "ctx", None),
            P(),
            P("fsdp", "ctx", None),
            P("fsdp"),
            P("fsdp", "tp"),
            P("fsdp", "tp"),
            P("fsdp", "tp"),
            P("fsdp"),
            P("fsdp"),
            P("tp", "fsdp"),
            P("fsdp"),
            P("fsdp", "tp"),
            P("fsdp", "tp"),
            P("tp", "fsdp"),
        ),
        check_vma=False,
    )
```

```python
import functools
import math

import jax
import jax.numpy as jnp
from jax import lax
from jax.experimental import pallas as pl
from jax.experimental.pallas import tpu as pltpu
from jax.sharding import PartitionSpec as P

EPS = 1e-05
THETA = 1000000.0
NEGATIVE = -1e30


def rms_scale(field_in, gain_vec):
    return (
        field_in * lax.rsqrt(jnp.mean(field_in * field_in, axis=-1, keepdims=True) + EPS) * gain_vec
    )


def rotate(field_in, positions):
    half_dim = field_in.shape[-1] // 2
    frequency = THETA ** (-(2.0 * jnp.arange(half_dim, dtype=jnp.float32)) / field_in.shape[-1])
    angles = positions[:, None] * frequency[None, :]
    cos_part = jnp.cos(angles)[:, None, :]
    sin_part = jnp.sin(angles)[:, None, :]
    lower_half = field_in[..., :half_dim]
    upper_half = field_in[..., half_dim:]
    return jnp.concatenate(
        [
            lower_half * cos_part - upper_half * sin_part,
            upper_half * cos_part + lower_half * sin_part,
        ],
        axis=-1,
    )


def linear(left_mat, right_mat):
    return jnp.dot(left_mat, right_mat, preferred_element_type=jnp.float32)


def linear_left(left_mat, right_mat):
    return lax.dot_general(
        left_mat, right_mat, (((0,), (0,)), ((), ())), preferred_element_type=jnp.float32
    )


def linear_right(left_mat, right_mat):
    return lax.dot_general(
        left_mat, right_mat, (((1,), (1,)), ((), ())), preferred_element_type=jnp.float32
    )


def swiglu(gate_act, up_act):
    return jax.nn.silu(gate_act) * up_act


def per_device_any(
    tokens,
    teacher,
    lengths,
    attn_gain,
    q_weight,
    k_weight,
    v_weight,
    q_gain,
    k_gain,
    o_weight,
    ffn_gain,
    gate_weight,
    up_weight,
    down_weight,
):
    (
        gain_one,
        w_query,
        w_key,
        w_value,
        gain_query,
        gain_key,
        w_output,
        gain_two,
        w_gate,
        w_upper,
        w_down,
    ) = (
        lax.all_gather(attn_gain, "fsdp", axis=0, tiled=True),
        lax.all_gather(q_weight, "fsdp", axis=0, tiled=True),
        lax.all_gather(k_weight, "fsdp", axis=0, tiled=True),
        lax.all_gather(v_weight, "fsdp", axis=0, tiled=True),
        lax.all_gather(q_gain, "fsdp", axis=0, tiled=True),
        lax.all_gather(k_gain, "fsdp", axis=0, tiled=True),
        lax.all_gather(o_weight, "fsdp", axis=1, tiled=True),
        lax.all_gather(ffn_gain, "fsdp", axis=0, tiled=True),
        lax.all_gather(gate_weight, "fsdp", axis=0, tiled=True),
        lax.all_gather(up_weight, "fsdp", axis=0, tiled=True),
        lax.all_gather(down_weight, "fsdp", axis=1, tiled=True),
    )
    rows_dev, block_len, model_width = tokens.shape
    count_tok = rows_dev * block_len
    head_dim = gain_query.shape[0]
    q_heads = w_query.shape[1] // head_dim
    kv_heads = w_key.shape[1] // head_dim
    group_size = q_heads // kv_heads
    score_scale = head_dim ** (-0.5)
    row_len = block_len * lax.axis_size("ctx")
    key_block = math.gcd(row_len, 512)
    block_start = lax.axis_index("ctx") * block_len
    tiles_used = (block_start + block_len + key_block - 1) // key_block
    slot_pos = block_start + jnp.arange(block_len, dtype=jnp.int32)
    positions = slot_pos.astype(jnp.float32)
    valid = (slot_pos[None, :] < lengths[:, None]).astype(jnp.float32)
    slots = count_tok * lax.axis_size("fsdp") * lax.axis_size("ctx")
    gain_two_f = gain_two.astype(jnp.float32)
    gain_one_f = gain_one.astype(jnp.float32)
    inputs = tokens.astype(jnp.float32)
    normed_one, back_one = jax.vjp(rms_scale, inputs, gain_one_f)
    normed_low = normed_one.astype(jnp.bfloat16).reshape(count_tok, model_width)
    query_raw = linear(normed_low, w_query)
    key_raw = linear(normed_low, w_key)
    value_raw = linear(normed_low, w_value)

    def heads_post(raw_heads, gain_vec):
        shaped = raw_heads.reshape(rows_dev, block_len, -1, head_dim)
        return rotate(rms_scale(shaped, gain_vec), positions)

    query_rot, query_back = jax.vjp(heads_post, query_raw, gain_query.astype(jnp.float32))
    key_rot, key_back = jax.vjp(heads_post, key_raw, gain_key.astype(jnp.float32))
    queries = query_rot.astype(jnp.bfloat16).reshape(
        rows_dev, block_len, kv_heads, group_size, head_dim
    )
    key_rows = key_rot.astype(jnp.bfloat16).reshape(rows_dev, block_len, kv_heads * head_dim)
    values = value_raw.astype(jnp.bfloat16).reshape(rows_dev, block_len, kv_heads * head_dim)
    keys_all, values_all = (
        lax.all_gather(key_rows, "ctx", axis=1, tiled=True),
        lax.all_gather(values, "ctx", axis=1, tiled=True),
    )

    def key_tile(tile_index):
        tile_start = tile_index * key_block
        key_pos = tile_start + jnp.arange(key_block, dtype=jnp.int32)
        key_part = lax.dynamic_slice_in_dim(keys_all, tile_start, key_block, 1).reshape(
            rows_dev, key_block, kv_heads, head_dim
        )
        value_part = lax.dynamic_slice_in_dim(values_all, tile_start, key_block, 1).reshape(
            rows_dev, key_block, kv_heads, head_dim
        )
        scores = (
            jnp.einsum("rqhgd,rkhd->rhgqk", queries, key_part, preferred_element_type=jnp.float32)
            * score_scale
        )
        allowed = (key_pos[None, None, :] <= slot_pos[None, :, None]) & (
            key_pos[None, None, :] < lengths[:, None, None]
        )
        return (tile_start, scores, allowed[:, None, None], key_part, value_part)

    stat_shape = (rows_dev, kv_heads, group_size, block_len)

    def stats_step(tile_index, carried):
        running_max, running_sum = carried
        tile_start, scores, allowed, key_part, value_part = key_tile(tile_index)
        masked = jnp.where(allowed, scores, NEGATIVE)
        new_max = jnp.maximum(running_max, jnp.max(masked, axis=-1))
        terms = jnp.where(allowed, jnp.exp(masked - new_max[..., None]), 0.0)
        return (new_max, running_sum * jnp.exp(running_max - new_max) + jnp.sum(terms, axis=-1))

    running_max, running_sum = lax.fori_loop(
        0,
        tiles_used,
        stats_step,
        (jnp.full(stat_shape, NEGATIVE, jnp.float32), jnp.zeros(stat_shape, jnp.float32)),
    )
    log_total = running_max + jnp.log(running_sum)
    out_shape = (rows_dev, block_len, kv_heads, group_size, head_dim)

    def value_step(tile_index, carried):
        rounded_out, exact_out = carried
        tile_start, scores, allowed, key_part, value_part = key_tile(tile_index)
        tile_probs = jnp.where(allowed, jnp.exp(scores - log_total[..., None]), 0.0)
        rounded_out = rounded_out + jnp.einsum(
            "rhgqk,rkhd->rqhgd",
            tile_probs.astype(jnp.bfloat16),
            value_part,
            preferred_element_type=jnp.float32,
        )
        exact_out = exact_out + jnp.einsum(
            "rhgqk,rkhd->rqhgd", tile_probs, value_part.astype(jnp.float32)
        )
        return (rounded_out, exact_out)

    rounded_out, exact_out = lax.fori_loop(
        0,
        tiles_used,
        value_step,
        (jnp.zeros(out_shape, jnp.float32), jnp.zeros(out_shape, jnp.float32)),
    )
    attended = rounded_out.astype(jnp.bfloat16).reshape(count_tok, q_heads * head_dim)
    attn_total = lax.psum(linear(attended, w_output), "tp")
    resid = inputs + attn_total.reshape(rows_dev, block_len, model_width)
    normed_two, back_two = jax.vjp(rms_scale, resid, gain_two_f)
    normed_second = normed_two.astype(jnp.bfloat16).reshape(count_tok, model_width)
    gate_act = linear(normed_second, w_gate)
    up_act = linear(normed_second, w_upper)
    hidden_full, back_glu = jax.vjp(swiglu, gate_act, up_act)
    hidden = hidden_full.astype(jnp.bfloat16)
    ffn_total = lax.psum(linear(hidden, w_down), "tp")
    result = resid + ffn_total.reshape(rows_dev, block_len, model_width)
    error_value = result - teacher.astype(jnp.float32)
    valid_col = valid[..., None]
    total_square, total_count = lax.psum(
        (jnp.sum(valid_col * error_value * error_value), jnp.sum(valid)), ("fsdp", "ctx")
    )
    teacher_loss = total_square / (total_count * model_width)
    grad_result = valid_col * error_value * (slots / total_count)
    grad_low = grad_result.astype(jnp.bfloat16).reshape(count_tok, model_width)
    grad_down = linear_left(hidden, grad_low)
    grad_hidden = linear_right(grad_low, w_down)
    grad_gate_full, grad_up_full = back_glu(grad_hidden)
    grad_gate = grad_gate_full.astype(jnp.bfloat16)
    grad_up = grad_up_full.astype(jnp.bfloat16)
    grad_wgate = linear_left(normed_second, grad_gate)
    grad_wup = linear_left(normed_second, grad_up)
    normed_two_part = linear_right(grad_gate, w_gate) + linear_right(grad_up, w_upper)
    grad_normed_two = lax.psum(normed_two_part, "tp")
    grad_resid_norm, grad_gain_two = back_two(
        grad_normed_two.reshape(rows_dev, block_len, model_width)
    )
    grad_resid = grad_result + grad_resid_norm
    grad_attn_low = grad_resid.astype(jnp.bfloat16).reshape(count_tok, model_width)
    grad_woutput = linear_left(attended, grad_attn_low)
    grad_attended = linear_right(grad_attn_low, w_output).astype(jnp.bfloat16).reshape(out_shape)
    delta = jnp.einsum("rqhgd,rqhgd->rhgq", grad_attended.astype(jnp.float32), exact_out)
    full_shape = (rows_dev, row_len, kv_heads * head_dim)

    def grad_step(tile_index, carried):
        grad_queries, grad_keys, grad_values = carried
        tile_start, scores, allowed, key_part, value_part = key_tile(tile_index)
        tile_probs = jnp.where(allowed, jnp.exp(scores - log_total[..., None]), 0.0)
        grad_probs = jnp.einsum(
            "rqhgd,rkhd->rhgqk", grad_attended, value_part, preferred_element_type=jnp.float32
        )
        grad_scores = (tile_probs * (grad_probs - delta[..., None])).astype(jnp.bfloat16)
        grad_queries = (
            grad_queries
            + jnp.einsum(
                "rhgqk,rkhd->rqhgd", grad_scores, key_part, preferred_element_type=jnp.float32
            )
            * score_scale
        )
        key_term = (
            jnp.einsum(
                "rhgqk,rqhgd->rkhd", grad_scores, queries, preferred_element_type=jnp.float32
            )
            * score_scale
        )
        value_term = jnp.einsum(
            "rhgqk,rqhgd->rkhd",
            tile_probs.astype(jnp.bfloat16),
            grad_attended,
            preferred_element_type=jnp.float32,
        )
        grad_keys = lax.dynamic_update_slice_in_dim(
            grad_keys, key_term.reshape(rows_dev, key_block, kv_heads * head_dim), tile_start, 1
        )
        grad_values = lax.dynamic_update_slice_in_dim(
            grad_values, value_term.reshape(rows_dev, key_block, kv_heads * head_dim), tile_start, 1
        )
        return (grad_queries, grad_keys, grad_values)

    grad_queries, grad_keys, grad_values = lax.fori_loop(
        0,
        tiles_used,
        grad_step,
        (
            jnp.zeros(out_shape, jnp.float32),
            jnp.zeros(full_shape, jnp.float32),
            jnp.zeros(full_shape, jnp.float32),
        ),
    )
    key_grad, value_grad = (
        lax.psum_scatter(grad_keys, "ctx", scatter_dimension=1, tiled=True),
        lax.psum_scatter(grad_values, "ctx", scatter_dimension=1, tiled=True),
    )
    grad_query_raw, grad_gain_query = query_back(
        grad_queries.reshape(rows_dev, block_len, q_heads, head_dim)
    )
    grad_key_raw, grad_gain_key = key_back(
        key_grad.reshape(rows_dev, block_len, kv_heads, head_dim)
    )
    query_low = grad_query_raw.astype(jnp.bfloat16)
    key_low = grad_key_raw.astype(jnp.bfloat16)
    value_low = value_grad.reshape(count_tok, kv_heads * head_dim).astype(jnp.bfloat16)
    grad_wquery = linear_left(normed_low, query_low)
    grad_wkey = linear_left(normed_low, key_low)
    grad_wvalue = linear_left(normed_low, value_low)
    normed_part = (
        linear_right(query_low, w_query)
        + linear_right(key_low, w_key)
        + linear_right(value_low, w_value)
    )
    grad_normed_one, grad_gain_query, grad_gain_key = lax.psum(
        (normed_part, grad_gain_query, grad_gain_key), "tp"
    )
    grad_input_norm, grad_gain_one = back_one(
        grad_normed_one.reshape(rows_dev, block_len, model_width)
    )
    tokens_grad = grad_resid + grad_input_norm
    partials = (
        grad_gain_one,
        grad_wquery,
        grad_wkey,
        grad_wvalue,
        grad_gain_query,
        grad_gain_key,
        grad_woutput,
        grad_gain_two,
        grad_wgate,
        grad_wup,
        grad_down,
    )
    pieces = (
        lax.psum_scatter(partials[0], ("fsdp", "ctx"), scatter_dimension=0, tiled=True),
        lax.psum_scatter(partials[1], ("fsdp", "ctx"), scatter_dimension=0, tiled=True),
        lax.psum_scatter(partials[2], ("fsdp", "ctx"), scatter_dimension=0, tiled=True),
        lax.psum_scatter(partials[3], ("fsdp", "ctx"), scatter_dimension=0, tiled=True),
        lax.psum_scatter(partials[4], ("fsdp", "ctx"), scatter_dimension=0, tiled=True),
        lax.psum_scatter(partials[5], ("fsdp", "ctx"), scatter_dimension=0, tiled=True),
        lax.psum_scatter(partials[6], ("fsdp", "ctx"), scatter_dimension=1, tiled=True),
        lax.psum_scatter(partials[7], ("fsdp", "ctx"), scatter_dimension=0, tiled=True),
        lax.psum_scatter(partials[8], ("fsdp", "ctx"), scatter_dimension=0, tiled=True),
        lax.psum_scatter(partials[9], ("fsdp", "ctx"), scatter_dimension=0, tiled=True),
        lax.psum_scatter(partials[10], ("fsdp", "ctx"), scatter_dimension=1, tiled=True),
    )
    summed = (
        lax.all_gather(pieces[0], "ctx", axis=0, tiled=True),
        lax.all_gather(pieces[1], "ctx", axis=0, tiled=True),
        lax.all_gather(pieces[2], "ctx", axis=0, tiled=True),
        lax.all_gather(pieces[3], "ctx", axis=0, tiled=True),
        lax.all_gather(pieces[4], "ctx", axis=0, tiled=True),
        lax.all_gather(pieces[5], "ctx", axis=0, tiled=True),
        lax.all_gather(pieces[6], "ctx", axis=1, tiled=True),
        lax.all_gather(pieces[7], "ctx", axis=0, tiled=True),
        lax.all_gather(pieces[8], "ctx", axis=0, tiled=True),
        lax.all_gather(pieces[9], "ctx", axis=0, tiled=True),
        lax.all_gather(pieces[10], "ctx", axis=1, tiled=True),
    )
    return (
        result.astype(jnp.bfloat16),
        teacher_loss,
        tokens_grad,
        summed[0],
        summed[1],
        summed[2],
        summed[3],
        summed[4],
        summed[5],
        summed[6],
        summed[7],
        summed[8],
        summed[9],
        summed[10],
    )


BF16 = jnp.bfloat16
F32 = jnp.float32
LOG2E = math.log2(math.e)
X_SWAP = [(0, 2), (2, 0), (1, 3), (3, 1)]
CORE_SWAP = [(0, 1), (1, 0), (2, 3), (3, 2)]
Y_SWAP = [(0, 1), (1, 0)]
Z_UP = [(0, 1), (1, 2), (2, 3), (3, 0)]
Z_DOWN = [(0, 3), (1, 0), (2, 1), (3, 2)]
Z_NEAR = [(0, 1), (1, 0), (2, 3), (3, 2)]
Z_FAR = [(0, 2), (2, 0), (1, 3), (3, 1)]
MASKS = (0, 2, 1, 3)
ANY = pl.BlockSpec(memory_space=pl.ANY)
SMEM = pl.BlockSpec(memory_space=pltpu.SMEM)


def fits(mesh):
    return dict(mesh.shape) == {"fsdp": 4, "ctx": 2, "tp": 4}


def dot(left, right, left_dim, right_dim):
    return lax.dot_general(
        left, right, (((left_dim,), (right_dim,)), ((), ())), preferred_element_type=F32
    )


def sigmoid(v):
    return 0.5 * jnp.tanh(0.5 * v) + 0.5


def whole(shape):
    zeros = (0,) * len(shape)
    return pl.BlockSpec(shape, lambda *_: zeros, pipeline_mode=pl.Buffered(1))


def settings(dims, mib):
    return pltpu.CompilerParams(
        dimension_semantics=("arbitrary",) * dims, vmem_limit_bytes=mib << 20
    )


def shape_of(shape, dtype):
    return jax.ShapeDtypeStruct(shape, dtype)


def cost(large):
    size = 1 << 42 if large else 1 << 10
    return pl.CostEstimate(flops=size, bytes_accessed=size >> 12, transcendentals=0)


def pack_kernel(info, o_in, g_in, u_in, d_in, *refs):
    out_ref, ffn_ref, *chunk_refs, others_ref, o_ref, g_ref, u_ref, d_ref, sems = refs
    ctx = info[2]
    pairs = ((o_in, o_ref), (g_in, g_ref), (u_in, u_ref), (d_in, d_ref))
    copies = [pltpu.make_async_copy(a, b, sems.at[i]) for i, (a, b) in enumerate(pairs)]
    for copy in copies:
        copy.start()
    for copy in copies:
        copy.wait()
    out_ref[...] = o_ref[...].astype(F32).T.astype(BF16)
    third = g_ref.shape[1] // 3
    for j in range(3):
        at = pl.multiple_of(jnp.where(ctx == 0, j, 2 - j) * third, third)
        parts = [
            g_ref[:, pl.ds(at, third)],
            u_ref[:, pl.ds(at, third)],
            d_ref[pl.ds(at, third), :].astype(F32).T.astype(BF16),
        ]
        for i, part in enumerate(parts):
            chunk_refs[j][:, i * third : (i + 1) * third] = part
            if j:
                others_ref[:, (3 * j - 3 + i) * third : (3 * j - 2 + i) * third] = part
            ffn_ref[:, (3 * j + i) * third : (3 * j + i + 1) * third] = part


def pack(info, o, g, u, d):
    rows, units = g.shape
    feats = o.shape[0]
    widths = (feats, 3 * units, units, units, units, 2 * units)
    return pl.pallas_call(
        pack_kernel,
        in_specs=[SMEM] + [ANY] * 4,
        out_specs=[pl.BlockSpec(memory_space=pltpu.VMEM)] * 6,
        out_shape=[shape_of((rows, n), BF16) for n in widths],
        scratch_shapes=[pltpu.VMEM(a.shape, BF16) for a in (o, g, u, d)]
        + [pltpu.SemaphoreType.DMA((4,))],
        compiler_params=pltpu.CompilerParams(vmem_limit_bytes=24 << 20),
        cost_estimate=cost(False),
        name="pack",
    )(info, o, g, u, d)


def join_kernel(q_ref, k_ref, v_ref, out_ref):
    at = 0
    for ref in (q_ref, k_ref, v_ref):
        out_ref[:, at : at + ref.shape[1]] = ref[...]
        at += ref.shape[1]


def join(q, k, v):
    return pl.pallas_call(
        join_kernel,
        out_shape=shape_of((q.shape[0], q.shape[1] + k.shape[1] + v.shape[1]), BF16),
        compiler_params=pltpu.CompilerParams(vmem_limit_bytes=8 << 20),
        cost_estimate=cost(False),
        name="join",
    )(q, k, v)


def norm_one_kernel(info, tok_ref, gain_ref, x_ref, nt_ref, x32):
    quarter = x_ref.shape[1] // 4
    for p, mask in enumerate(MASKS):
        at = pl.multiple_of(jnp.bitwise_xor(info[1], mask) * quarter, quarter)
        part = tok_ref[0, :, pl.ds(at, quarter)]
        x_ref[:, p * quarter : (p + 1) * quarter] = part
        x32[:, p * quarter : (p + 1) * quarter] = part.astype(F32)
    x = x32[...]
    rho = lax.rsqrt(jnp.mean(x * x, axis=-1, keepdims=True) + EPS)
    nt_ref[...] = (x * rho * gain_ref[...]).T.astype(BF16)


def norm_one(info, tokens, gain, tile):
    _, tok, width = tokens.shape
    return pl.pallas_call(
        norm_one_kernel,
        grid_spec=pltpu.PrefetchScalarGridSpec(
            num_scalar_prefetch=1,
            grid=(tok // tile,),
            in_specs=[
                pl.BlockSpec((1, tile, width), lambda i, info: (info[0], i, 0)),
                pl.BlockSpec((1, width), lambda i, info: (0, 0)),
            ],
            out_specs=[
                pl.BlockSpec((tile, width), lambda i, info: (i, 0)),
                pl.BlockSpec((width, tile), lambda i, info: (0, i)),
            ],
            scratch_shapes=[pltpu.VMEM((tile, width), F32)],
        ),
        out_shape=[shape_of((tok, width), BF16), shape_of((width, tok), BF16)],
        compiler_params=settings(1, 24),
        cost_estimate=cost(False),
        name="norm_one",
    )(info, tokens, gain)


def proj_kernel(heads, block, plan, count, info, *refs):
    nt_ref, cos_ref, sin_ref, qg_ref, kg_ref, rot_ref, raw_ref, w_ref, sem = refs[count:]
    rows = w_ref.shape[0] // 4

    @pl.when(pl.program_id(0) == 0)
    def _():
        for k in range(4):

            @pl.when(block(info) == k)
            def _():
                for p, (piece, row) in enumerate(plan[k]):
                    src = refs[piece].at[pl.ds(row, rows)]
                    pltpu.make_async_copy(src, w_ref.at[pl.ds(p * rows, rows)], sem).start()

        pltpu.make_async_copy(w_ref, w_ref, sem).wait()

    hd = qg_ref.shape[0]
    half = hd // 2
    raw = dot(w_ref[...], nt_ref[...], 0, 0)
    cos_part, sin_part = cos_ref[...], sin_ref[...]
    heads_q, heads_k = heads
    raw_ref[...] = raw.astype(BF16)
    for h in range(heads_q + heads_k):
        v = raw[h * hd : (h + 1) * hd]
        rho = lax.rsqrt(jnp.mean(v * v, axis=0, keepdims=True) + EPS)
        v = v * rho * (qg_ref[...] if h < heads_q else kg_ref[...])
        a, b = v[:half], v[half:]
        rot_ref[h * hd : h * hd + half, :] = (a * cos_part - b * sin_part).astype(BF16)
        rot_ref[h * hd + half : (h + 1) * hd, :] = (b * cos_part + a * sin_part).astype(BF16)
    at = (heads_q + heads_k) * hd
    rot_ref[at:, :] = raw[at:].astype(BF16)


def project(info, weights, normed_t, cos_part, sin_part, gain_q, gain_k, heads, block):
    plan, pieces = weights
    width, tok = normed_t.shape
    cols = pieces[0].shape[1]
    tile = min(512, tok)
    const = lambda a: pl.BlockSpec(a.shape, lambda i, info: (0, 0))
    tab = lambda a: pl.BlockSpec((a.shape[0], tile), lambda i, info: (0, i))
    return pl.pallas_call(
        functools.partial(proj_kernel, heads, block, plan, len(pieces)),
        grid_spec=pltpu.PrefetchScalarGridSpec(
            num_scalar_prefetch=1,
            grid=(tok // tile,),
            in_specs=[ANY] * len(pieces)
            + [tab(normed_t), tab(cos_part), tab(sin_part), const(gain_q), const(gain_k)],
            out_specs=[pl.BlockSpec((cols, tile), lambda i, info: (0, i))] * 2,
            scratch_shapes=[pltpu.VMEM((width, cols), BF16), pltpu.SemaphoreType.DMA],
        ),
        out_shape=[shape_of((cols, tok), BF16), shape_of((cols, tok), BF16)],
        compiler_params=settings(1, 24),
        cost_estimate=cost(False),
        name="project",
    )(info, *pieces, normed_t, cos_part, sin_part, gain_q, gain_k)


def head_back_kernel(
    heads, info, dm_ref, dt_ref, rm_ref, rt_ref, cos_ref, sin_ref, qg_ref, kg_ref, out_ref, gg_ref
):
    step, part = pl.program_id(0), pl.program_id(1)
    hd = qg_ref.shape[0]
    half = hd // 2
    heads_q, heads_k = heads
    cos_part, sin_part = cos_ref[...], sin_ref[...]
    tile = cos_part.shape[1]

    @pl.when((step == 0) & (part == 0))
    def _():
        gg_ref[...] = jnp.zeros_like(gg_ref)

    def work(d_ref, r_ref):
        gain_q = jnp.zeros((hd, 1), F32)
        gain_k = jnp.zeros((hd, 1), F32)
        done = []
        for h in range(heads_q + heads_k):
            is_q = h < heads_q
            g = d_ref[h * hd : (h + 1) * hd, :].astype(F32)
            raw = r_ref[h * hd : (h + 1) * hd, :].astype(F32)
            a, b = g[:half], g[half:]
            turned = jnp.concatenate(
                [a * cos_part + b * sin_part, b * cos_part - a * sin_part], axis=0
            )
            rho = lax.rsqrt(jnp.mean(raw * raw, axis=0, keepdims=True) + EPS)
            unit = raw * rho
            prod = turned * unit
            scaled = turned * (qg_ref[...] if is_q else kg_ref[...])
            mean = jnp.mean(scaled * unit, axis=0, keepdims=True)
            done.append(rho * (scaled - unit * mean))
            total = jnp.sum(prod, axis=1, keepdims=True)
            if is_q:
                gain_q = gain_q + total
            else:
                gain_k = gain_k + total
        done.append(d_ref[(heads_q + heads_k) * hd :, :].astype(F32))
        out_ref[0] = jnp.concatenate(done, axis=0).T.astype(BF16)
        lane = lax.broadcasted_iota(jnp.int32, gg_ref.shape, 1)
        gg_ref[...] += jnp.where(lane == 0, gain_q, jnp.where(lane == 1, gain_k, 0.0))

    @pl.when(step == 0)
    def _():
        work(dm_ref, rm_ref)

    @pl.when(step == 1)
    def _():
        work(dt_ref, rt_ref)


def head_back(info, grad_mine, grad_theirs, raw_mine, raw_theirs, cos_part, sin_part, gq, gk, heads):
    cols, tok = grad_mine.shape
    tile = min(512, tok)
    mine = pl.BlockSpec((cols, tile), lambda s, i, info: (0, jnp.where(s == 0, i, tok // tile - 1)))
    theirs = pl.BlockSpec((cols, tile), lambda s, i, info: (0, jnp.where(s == 0, 0, i)))
    tab = lambda a: pl.BlockSpec((a.shape[0], tile), lambda s, i, info: (0, i))
    const = lambda a: pl.BlockSpec(a.shape, lambda s, i, info: (0, 0))
    return pl.pallas_call(
        functools.partial(head_back_kernel, heads),
        grid_spec=pltpu.PrefetchScalarGridSpec(
            num_scalar_prefetch=1,
            grid=(2, tok // tile),
            in_specs=[
                mine,
                theirs,
                mine,
                theirs,
                tab(cos_part),
                tab(sin_part),
                const(gq),
                const(gk),
            ],
            out_specs=[
                pl.BlockSpec(
                    (1, tile, cols), lambda s, i, info: (jnp.bitwise_xor(info[2], s), i, 0)
                ),
                pl.BlockSpec((gq.shape[0], 128), lambda s, i, info: (0, 0)),
            ],
        ),
        out_shape=[shape_of((2, tok, cols), BF16), shape_of((gq.shape[0], 128), F32)],
        compiler_params=settings(2, 60),
        cost_estimate=cost(False),
        name="head_back",
    )(info, grad_mine, grad_theirs, raw_mine, raw_theirs, cos_part, sin_part, gq, gk)


def load_rows(info, mine_ref, got_ref, rows, sems):
    tok = mine_ref.shape[1]
    ctx = info[2]
    here = pl.multiple_of(ctx * tok, tok)
    there = pl.multiple_of((1 - ctx) * tok, tok)
    one = pltpu.make_async_copy(mine_ref, rows.at[:, pl.ds(here, tok)], sems.at[0])
    two = pltpu.make_async_copy(got_ref, rows.at[:, pl.ds(there, tok)], sems.at[1])
    one.start()
    two.start()
    one.wait()
    two.wait()


def keys_with_bias(keys, length):
    hd, slots = keys.shape
    pos = lax.broadcasted_iota(jnp.int32, (hd, slots), 1)
    row = lax.broadcasted_iota(jnp.int32, (hd, slots), 0)
    bias = jnp.where((row == 0) & (pos >= length), NEGATIVE, 0.0)
    return jnp.concatenate([keys.astype(F32), bias], axis=0).T.astype(BF16)


def query_with_one(pair):
    one_row = jnp.where(lax.broadcasted_iota(jnp.int32, pair.shape, 0) == 0, 1.0, 0.0)
    return jnp.concatenate([pair, one_row.astype(BF16)], axis=0)


def by_halves(left, right):
    half = left.shape[1] // 2
    return jnp.concatenate(
        [left[:, :half], right[:, :half], left[:, half:], right[:, half:]], axis=1
    )


def by_heads(both):
    quarter = both.shape[1] // 4
    part = lambda i: both[:, i * quarter : (i + 1) * quarter]
    return (
        jnp.concatenate([part(0), part(2)], axis=1),
        jnp.concatenate([part(1), part(3)], axis=1),
    )


def causal(scores):
    half = scores.shape[0]
    key_pos = lax.broadcasted_iota(jnp.int32, (half, half), 0)
    query_pos = lax.broadcasted_iota(jnp.int32, (half, half), 1)
    allowed = key_pos <= query_pos
    return jnp.where(jnp.concatenate([allowed, allowed], axis=1), scores, NEGATIVE)


def attn_fwd_kernel(
    width, hd, info, mine_ref, got_ref, keep_ref, send_ref, lse_ref, rows, key_rows, sems
):
    head, block = pl.program_id(0), pl.program_id(1)
    heads_k = pl.num_programs(0)
    scale = hd**-0.5 * LOG2E
    length = info[3]
    key_at = pl.multiple_of(heads_k * 2 * hd + head * hd, hd)
    value_at = pl.multiple_of(heads_k * 3 * hd + head * hd, hd)
    query_at = pl.multiple_of(head * 2 * hd, 2 * hd)

    @pl.when((head == 0) & (block == 0))
    def _():
        load_rows(info, mine_ref, got_ref, rows, sems)

    @pl.when(block == 0)
    def _():
        key_rows[...] = keys_with_bias(rows[pl.ds(key_at, hd), :], length)

    start = pl.multiple_of(block * width, width)
    both = rows[pl.ds(query_at, 2 * hd), pl.ds(start, width)]
    query = query_with_one(by_halves(both[:hd], both[hd:]))

    def tile(at, carried, diagonal):
        out, total = carried
        scores = dot(key_rows[pl.ds(at, width), :], query, 1, 0)
        if diagonal:
            key_pos = lax.broadcasted_iota(jnp.int32, (width, width), 0)
            query_pos = lax.broadcasted_iota(jnp.int32, (width, width), 1)
            allowed = key_pos <= query_pos
            allowed = by_halves(allowed, allowed)
            scores = jnp.where(allowed, scores, NEGATIVE)
        probs = jnp.exp2(scores * scale)
        total = total + jnp.sum(probs, axis=0, keepdims=True)
        out = out + dot(rows[pl.ds(value_at, hd), pl.ds(at, width)], probs.astype(BF16), 1, 0)
        return out, total

    carried = (jnp.zeros((hd, 2 * width), F32), jnp.zeros((1, 2 * width), F32))
    full = jnp.minimum(block, lax.div(length + width - 1, width))
    carried = lax.fori_loop(
        0, full, lambda j, c: tile(pl.multiple_of(j * width, width), c, False), carried
    )
    out, total = tile(start, carried, True)
    out = out * (1.0 / total)
    out = jnp.concatenate(by_heads(out), axis=0).T.astype(BF16)
    here = block // 2 == info[2]

    @pl.when(here)
    def _():
        keep_ref[...] = out

    @pl.when(jnp.logical_not(here))
    def _():
        send_ref[...] = out

    log_first, log_second = by_heads(jnp.log2(total))
    lse_ref[0, 0:1, :] = log_first
    lse_ref[0, 1:2, :] = log_second


def keep_block(i, info):
    return jnp.clip(i - 2 * info[2], 0, 1)


def send_block(i, info):
    return jnp.clip(i - 2 * (1 - info[2]), 0, 1)


def attn_fwd(info, mine, got, hd):
    cols, tok = mine.shape
    heads_k = cols // (4 * hd)
    width = tok // 2
    return pl.pallas_call(
        functools.partial(attn_fwd_kernel, width, hd),
        grid_spec=pltpu.PrefetchScalarGridSpec(
            num_scalar_prefetch=1,
            grid=(heads_k, 4),
            in_specs=[ANY, ANY],
            out_specs=[
                pl.BlockSpec((width, 2 * hd), lambda h, i, info: (keep_block(i, info), h)),
                pl.BlockSpec((width, 2 * hd), lambda h, i, info: (send_block(i, info), h)),
                pl.BlockSpec((1, 2, width), lambda h, i, info: (h, 0, i)),
            ],
            scratch_shapes=[
                pltpu.VMEM((cols, 2 * tok), BF16),
                pltpu.VMEM((2 * tok, 2 * hd), BF16),
                pltpu.SemaphoreType.DMA((2,)),
            ],
        ),
        out_shape=[
            shape_of((tok, heads_k * 2 * hd), BF16),
            shape_of((tok, heads_k * 2 * hd), BF16),
            shape_of((heads_k, 2, 2 * tok), F32),
        ],
        compiler_params=settings(2, 60),
        cost_estimate=cost(True),
        name="attn_fwd",
    )(info, mine, got)


def attn_bwd_kernel(
    width,
    hd,
    info,
    mine_ref,
    got_ref,
    ok_ref,
    os_ref,
    gk_ref,
    gs_ref,
    lse_ref,
    keep_ref,
    send_ref,
    rows,
    key_rows,
    value_rows,
    key_sum,
    value_sum,
    sems,
):
    head, block = pl.program_id(0), pl.program_id(1)
    heads_k = pl.num_programs(0)
    scale = hd**-0.5
    length = info[3]
    ctx = info[2]
    tok = keep_ref.shape[1]
    key_at = pl.multiple_of(heads_k * 2 * hd + head * hd, hd)
    value_at = pl.multiple_of(heads_k * 3 * hd + head * hd, hd)
    query_at = pl.multiple_of(head * 2 * hd, 2 * hd)

    @pl.when((head == 0) & (block == 0))
    def _():
        load_rows(info, mine_ref, got_ref, rows, sems)

    @pl.when(block == 0)
    def _():
        key_rows[...] = keys_with_bias(rows[pl.ds(key_at, hd), :], length)
        value_rows[...] = rows[pl.ds(value_at, hd), :].astype(F32).T.astype(BF16)
        key_sum[...] = jnp.zeros_like(key_sum)
        value_sum[...] = jnp.zeros_like(value_sum)

    start = pl.multiple_of(block * width, width)
    here = block // 2 == ctx

    def store_query(value):
        at = pl.ds(pl.multiple_of((block % 2) * width, width), width)

        @pl.when(here)
        def _():
            keep_ref[pl.ds(query_at, 2 * hd), at] = value

        @pl.when(jnp.logical_not(here))
        def _():
            send_ref[pl.ds(query_at, 2 * hd), at] = value

    @pl.when(block * width < length)
    def _():
        both = rows[pl.ds(query_at, 2 * hd), pl.ds(start, width)]
        pair = by_halves(both[:hd], both[hd:])
        query = query_with_one(pair)
        query_rows = pair.astype(F32).T.astype(BF16)
        grad_wide = jnp.where(here, gk_ref[...].astype(F32), gs_ref[...].astype(F32))
        out_wide = jnp.where(here, ok_ref[...].astype(F32), os_ref[...].astype(F32))
        grad_t = grad_wide.T
        prod = (grad_wide * out_wide).T
        grad = by_halves(grad_t[:hd], grad_t[hd:]).astype(BF16)
        half = width // 2
        grad_rows = jnp.concatenate(
            [
                grad_wide[:half, :hd],
                grad_wide[:half, hd:],
                grad_wide[half:, :hd],
                grad_wide[half:, hd:],
            ],
            axis=0,
        ).astype(BF16)
        delta = by_halves(
            jnp.sum(prod[:hd], axis=0, keepdims=True), jnp.sum(prod[hd:], axis=0, keepdims=True)
        )
        lse = by_halves(lse_ref[0, 0:1, :], lse_ref[0, 1:2, :])

        def terms(at, keys, first, mask):
            scores = dot(key_rows[pl.ds(at, keys), :], query[:, first:], 1, 0)
            if mask:
                part = causal(scores[:, :width])
                wide = scores.shape[1] > width
                scores = jnp.concatenate([part, scores[:, width:]], axis=1) if wide else part
            probs = jnp.exp2(scores * (scale * LOG2E) - lse[:, first:])
            grad_probs = dot(value_rows[pl.ds(at, keys), :], grad[:, first:], 1, 0)
            grad_scores = (probs * (grad_probs - delta[:, first:])).astype(BF16)
            value_sum[pl.ds(at, keys), :] += dot(probs.astype(BF16), grad_rows[first:], 1, 0)
            key_sum[pl.ds(at, keys), :] += dot(grad_scores, query_rows[first:], 1, 0)
            return dot(rows[pl.ds(key_at, hd), pl.ds(at, keys)], grad_scores, 1, 0)

        query_sum = lax.fori_loop(
            0,
            block,
            lambda j, s: s + terms(pl.multiple_of(j * width, width), width, 0, False),
            jnp.zeros((hd, 2 * width), F32),
        )
        query_sum = query_sum + terms(start, half, 0, True)
        later = terms(pl.multiple_of(start + half, half), half, width, True)
        query_sum = jnp.concatenate([query_sum[:, :width], query_sum[:, width:] + later], axis=1)
        store_query(jnp.concatenate(by_heads(query_sum * scale), axis=0).astype(BF16))

    @pl.when(block * width >= length)
    def _():
        store_query(jnp.zeros((2 * hd, width), BF16))

    @pl.when(block == 3)
    def _():
        for at, total in ((key_at, key_sum[...] * scale), (value_at, value_sum[...])):
            total = total.T.astype(BF16)
            left, right = total[:, :tok], total[:, tok:]

            @pl.when(ctx == 0)
            def _():
                keep_ref[pl.ds(at, hd), :] = left
                send_ref[pl.ds(at, hd), :] = right

            @pl.when(ctx == 1)
            def _():
                keep_ref[pl.ds(at, hd), :] = right
                send_ref[pl.ds(at, hd), :] = left


def attn_bwd(info, mine, got, out_keep, out_send, grad_keep, grad_send, lse, hd):
    cols, tok = mine.shape
    heads_k = cols // (4 * hd)
    width = tok // 2
    keep = pl.BlockSpec((width, 2 * hd), lambda h, i, info: (keep_block(i, info), h))
    send = pl.BlockSpec((width, 2 * hd), lambda h, i, info: (send_block(i, info), h))
    full = pl.BlockSpec((cols, tok), lambda h, i, info: (0, 0))
    return pl.pallas_call(
        functools.partial(attn_bwd_kernel, width, hd),
        grid_spec=pltpu.PrefetchScalarGridSpec(
            num_scalar_prefetch=1,
            grid=(heads_k, 4),
            in_specs=[
                ANY,
                ANY,
                keep,
                send,
                keep,
                send,
                pl.BlockSpec((1, 2, width), lambda h, i, info: (h, 0, i)),
            ],
            out_specs=[full, full],
            scratch_shapes=[
                pltpu.VMEM((cols, 2 * tok), BF16),
                pltpu.VMEM((2 * tok, 2 * hd), BF16),
                pltpu.VMEM((2 * tok, hd), BF16),
                pltpu.VMEM((2 * tok, hd), F32),
                pltpu.VMEM((2 * tok, hd), F32),
                pltpu.SemaphoreType.DMA((2,)),
            ],
        ),
        out_shape=[shape_of((cols, tok), BF16), shape_of((cols, tok), BF16)],
        compiler_params=settings(2, 60),
        cost_estimate=cost(True),
        name="attn_bwd",
    )(info, mine, got, out_keep, out_send, grad_keep, grad_send, lse)


def load_blocks(plan, pieces, target, sem):
    rows = target.shape[1] // 4

    @pl.when(pl.program_id(0) == 0)
    def _():
        for k, places in enumerate(plan):
            for p, (piece, row) in enumerate(places):
                src = pieces[piece].at[pl.ds(row, rows)]
                pltpu.make_async_copy(src, target.at[k, pl.ds(p * rows, rows)], sem).start()
        pltpu.make_async_copy(target, target, sem).wait()


def out_proj_kernel(plan, count, info, *refs):
    x_ref, a0, a1, b0, b1, gain_ref, r_ref, n_ref, nt_ref, att_ref, w_ref, sem = refs[count:]
    load_blocks(plan, refs, w_ref, sem)
    ctx = info[2]
    total = x_ref[...].astype(F32)
    for j, ref, side in ((0, a0, ctx), (1, a1, ctx), (0, b0, 1 - ctx), (1, b1, 1 - ctx)):
        block = 2 * side + j
        part = ref[...]
        att_ref[block] = part
        total = total + dot(part, w_ref[block], 1, 1)
    rho = lax.rsqrt(jnp.mean(total * total, axis=-1, keepdims=True) + EPS)
    normed = total * rho * gain_ref[...]
    r_ref[...] = total
    n_ref[...] = normed.astype(BF16)
    nt_ref[...] = normed.T.astype(BF16)


def out_proj(info, x, mine, theirs, weights, gain, tile):
    plan, pieces = weights
    tok, width = x.shape
    feats = pieces[0].shape[1]
    rows_of = lambda n: pl.BlockSpec((tile, n), lambda i, info: (i, 0))
    return pl.pallas_call(
        functools.partial(out_proj_kernel, plan, len(pieces)),
        grid_spec=pltpu.PrefetchScalarGridSpec(
            num_scalar_prefetch=1,
            grid=(tok // tile,),
            in_specs=[ANY] * len(pieces)
            + [rows_of(width)]
            + [rows_of(feats)] * 4
            + [pl.BlockSpec((1, width), lambda i, info: (0, 0))],
            out_specs=[
                rows_of(width),
                rows_of(width),
                pl.BlockSpec((width, tile), lambda i, info: (0, i)),
                pl.BlockSpec((4, tile, feats), lambda i, info: (0, i, 0)),
            ],
            scratch_shapes=[pltpu.VMEM((4, width, feats), BF16), pltpu.SemaphoreType.DMA],
        ),
        out_shape=[
            shape_of((tok, width), F32),
            shape_of((tok, width), BF16),
            shape_of((width, tok), BF16),
            shape_of((4, tok, feats), BF16),
        ],
        compiler_params=settings(1, 60),
        cost_estimate=cost(True),
        name="out_proj",
    )(info, *pieces, x, *mine, *theirs, gain)


def norm_two_back_kernel(plan, count, info, *refs):
    g_ref, r_ref, gr_ref, gain_ref, gres_ref, gat_ref, a0, a1, b0, b1, gg_ref, w_ref, sem = refs[count:]
    load_blocks(plan, refs, w_ref, sem)
    ctx = info[2]
    grad, resid = g_ref[...], r_ref[...]
    rho = lax.rsqrt(jnp.mean(resid * resid, axis=-1, keepdims=True) + EPS)
    unit = resid * rho
    scaled = grad * gain_ref[...]
    back = rho * (scaled - unit * jnp.mean(scaled * unit, axis=-1, keepdims=True))
    total = gr_ref[...] + back
    gres_ref[...] = total
    low = total.astype(BF16)
    gat_ref[...] = total.T.astype(BF16)

    @pl.when(pl.program_id(0) == 0)
    def _():
        gg_ref[...] = jnp.zeros_like(gg_ref)

    gg_ref[...] += jnp.sum(grad * unit, axis=0, keepdims=True)
    for j, ref, side in ((0, a0, ctx), (1, a1, ctx), (0, b0, 1 - ctx), (1, b1, 1 - ctx)):
        ref[...] = dot(low, w_ref[2 * side + j], 1, 0).astype(BF16)


def norm_two_back(info, grad, resid, grad_result, gain, weights, tile):
    plan, pieces = weights
    tok, width = grad.shape
    feats = pieces[0].shape[1]
    rows_of = lambda n: pl.BlockSpec((tile, n), lambda i, info: (i, 0))
    row = pl.BlockSpec((1, width), lambda i, info: (0, 0))
    return pl.pallas_call(
        functools.partial(norm_two_back_kernel, plan, len(pieces)),
        grid_spec=pltpu.PrefetchScalarGridSpec(
            num_scalar_prefetch=1,
            grid=(tok // tile,),
            in_specs=[ANY] * len(pieces) + [rows_of(width)] * 3 + [row],
            out_specs=[rows_of(width), pl.BlockSpec((width, tile), lambda i, info: (0, i))]
            + [rows_of(feats)] * 4
            + [row],
            scratch_shapes=[pltpu.VMEM((4, width, feats), BF16), pltpu.SemaphoreType.DMA],
        ),
        out_shape=[shape_of((tok, width), F32), shape_of((width, tok), BF16)]
        + [shape_of((tok, feats), BF16)] * 4
        + [shape_of((1, width), F32)],
        compiler_params=settings(1, 60),
        cost_estimate=cost(True),
        name="norm_two_back",
    )(info, *pieces, grad, resid, grad_result, gain)


def norm_one_back_kernel(plan, count, info, *refs):
    p0, p1, x_ref, gres_ref, gain_ref, out_ref, gg_ref, w_ref, sem = refs[count:]
    load_blocks(plan, refs, w_ref, sem)
    quarter = x_ref.shape[1] // 4
    grad = dot(p0[0], w_ref[0], 1, 1)
    grad = grad + dot(p1[0], w_ref[1], 1, 1)
    grad = grad + dot(p0[1], w_ref[2], 1, 1)
    grad = grad + dot(p1[1], w_ref[3], 1, 1)
    x = x_ref[...].astype(F32)
    rho = lax.rsqrt(jnp.mean(x * x, axis=-1, keepdims=True) + EPS)
    unit = x * rho
    scaled = grad * gain_ref[...]
    back = rho * (scaled - unit * jnp.mean(scaled * unit, axis=-1, keepdims=True))
    total = (gres_ref[...] + back).astype(BF16)
    for p, mask in enumerate(MASKS):
        at = pl.multiple_of(jnp.bitwise_xor(info[1], mask) * quarter, quarter)
        part = total[:, p * quarter : (p + 1) * quarter]

        out_ref[:, pl.ds(at, quarter)] = part

    @pl.when(pl.program_id(0) == 0)
    def _():
        gg_ref[...] = jnp.zeros_like(gg_ref)

    gg_ref[...] += jnp.sum(grad * unit, axis=0, keepdims=True)


def norm_one_back(info, pairs, weights, x, grad_resid, gain, tile, part):
    plan, pieces = weights
    tok, width = x.shape
    cols = pieces[0].shape[1]
    steps = tok // tile // 2
    first = part * steps
    rows_of = lambda n: pl.BlockSpec((tile, n), lambda i, info: (first + i, 0))
    out_rows = pl.BlockSpec((tile, width), lambda i, info: (i, 0))
    pair = pl.BlockSpec((2, tile, cols), lambda i, info: (0, first + i, 0))
    row = pl.BlockSpec((1, width), lambda i, info: (0, 0))
    return pl.pallas_call(
        functools.partial(norm_one_back_kernel, plan, len(pieces)),
        grid_spec=pltpu.PrefetchScalarGridSpec(
            num_scalar_prefetch=1,
            grid=(steps,),
            in_specs=[ANY] * len(pieces) + [pair, pair, rows_of(width), rows_of(width), row],
            out_specs=[out_rows, row],
            scratch_shapes=[pltpu.VMEM((4, width, cols), BF16), pltpu.SemaphoreType.DMA],
        ),
        out_shape=[shape_of((tok // 2, width), BF16), shape_of((1, width), F32)],
        compiler_params=settings(1, 60),
        cost_estimate=cost(True),
        name="norm_one_back",
    )(info, *pieces, *pairs, x, grad_resid, gain)


def weight_copies(plan, pieces, gate_up, down, gate_up_sem, down_sem):
    third = down.shape[1] // 3
    rows = down.shape[0] // 4
    wide, thin = [], []
    for p, chunks in enumerate(plan):
        block = pl.ds(p * rows, rows)
        for j, (piece, row, at) in enumerate(chunks):
            src = pieces[piece].at[pl.ds(row, rows)]
            wide.append(
                pltpu.make_async_copy(
                    src.at[:, pl.ds(at, 2 * third)],
                    gate_up.at[block, pl.ds(j * 2 * third, 2 * third)],
                    gate_up_sem,
                )
            )
            thin.append(
                pltpu.make_async_copy(
                    src.at[:, pl.ds(at + 2 * third, third)],
                    down.at[block, pl.ds(j * third, third)],
                    down_sem,
                )
            )
    return wide, thin


def split_act(act):
    third = act.shape[1] // 6
    part = lambda j: act[:, j * third : (j + 1) * third]
    return [(part(0), part(1)), (part(2), part(3)), (part(4), part(5))]


def ffn_fwd_kernel(tile, plans, last, info, scale, x_ref, in_ref, *rest):
    if last:
        teach_ref, rest = rest[0], rest[1:]
    pieces = []
    for plan in plans:
        count = 1 + max(place[0] for chunks in plan for place in chunks)
        pieces.append(rest[:count])
        rest = rest[count:]
    act_ref, hid_ref = rest[:2]
    if last:
        outa_ref, outb_ref, gres_ref, low_ref, lowt_ref, sq_ref = rest[2:8]
        gate_up, down, total, sems = rest[8:]
    else:
        sum_ref, gate_up, down, total, sems = rest[2:]
    step, part = pl.program_id(0), pl.program_id(1)
    final = len(plans) - 1
    width = x_ref.shape[1]
    quarter = width // 4
    third = down.shape[2] // 3

    def copies(s):
        return weight_copies(
            plans[s], pieces[s], gate_up.at[s], down.at[s], sems.at[s, 0], sems.at[s, 1]
        )

    @pl.when((step == 0) & (part == 0))
    def _():
        for s in range(len(plans)):
            wide, thin = copies(s)
            for copy in wide + thin:
                copy.start()

    for s in range(len(plans)):

        @pl.when((step == s) & (part == 0))
        def _():
            pltpu.make_async_copy(gate_up.at[s], gate_up.at[s], sems.at[s, 0]).wait()

    rows = pl.ds(pl.multiple_of(part * tile, tile), tile)
    act = dot(x_ref[rows, :], gate_up[step], 1, 0)
    for j, (gate, upper) in enumerate(split_act(act)):
        sig = sigmoid(gate)
        silu = gate * sig
        hid_ref[0, :, j * third : (j + 1) * third] = (silu * upper).astype(BF16)
        at = 2 * j * third
        act_ref[0, :, at : at + third] = (upper * (sig + silu - silu * sig)).astype(BF16)
        act_ref[0, :, at + third : at + 2 * third] = silu.astype(BF16)
    for s in range(len(plans)):

        @pl.when((step == s) & (part == 0))
        def _():
            pltpu.make_async_copy(down.at[s], down.at[s], sems.at[s, 1]).wait()

    grown = dot(hid_ref[0], down[step], 1, 1)

    @pl.when(step == 0)
    def _():
        total[rows, :] = in_ref[...] + grown

    @pl.when(step > 0)
    def _():
        total[rows, :] += grown

    @pl.when(step == final)
    def _():
        result = total[rows, :]
        if not last:
            sum_ref[...] = result
            return
        tok = x_ref.shape[0]
        slot = info[2] * tok + part * tile + lax.broadcasted_iota(jnp.int32, (tile, 1), 0)
        valid = jnp.where(slot < info[3], 1.0, 0.0)
        square = jnp.zeros((tile, quarter), F32)
        for p, mask in enumerate(MASKS):
            at = pl.multiple_of(jnp.bitwise_xor(info[1], mask) * quarter, quarter)
            cols = slice(p * quarter, (p + 1) * quarter)
            value = result[:, cols]
            low = value.astype(BF16)

            @pl.when(part < pl.num_programs(1) // 2)
            def _():
                outa_ref[:, pl.ds(at, quarter)] = low

            @pl.when(part >= pl.num_programs(1) // 2)
            def _():
                outb_ref[:, pl.ds(at, quarter)] = low

            error = valid * (value - teach_ref[0, :, pl.ds(at, quarter)].astype(F32))
            square = square + error * error
            grad = error * scale[0]
            gres_ref[:, cols] = grad
            low_ref[:, cols] = grad.astype(BF16)
            lowt_ref[cols, :] = grad.T.astype(BF16)

        @pl.when(part == 0)
        def _():
            sq_ref[...] = jnp.zeros_like(sq_ref)

        sq_ref[...] += jnp.sum(square, axis=0, keepdims=True)


def ffn_fwd(info, scale, x, total, teacher, weights, units, tile):
    tok, width = x.shape
    pieces = [piece for _, group in weights for piece in group]
    count = len(weights)
    last = teacher is not None
    entry = lambda s, i: jnp.where(s == 0, i, tok // tile - 1)
    leave = lambda s, i: jnp.where(s == count - 1, i, 0)
    tiles = lambda n: pl.BlockSpec((tile, n), lambda s, i, info: (leave(s, i), 0))
    slab = lambda n: pl.BlockSpec((1, tile, n), lambda s, i, info: (s, i, 0))
    in_specs = [
        SMEM,
        whole((tok, width)),
        pl.BlockSpec((tile, width), lambda s, i, info: (entry(s, i), 0)),
    ]
    out_specs = [slab(2 * units), slab(units)]
    out_shape = [shape_of((count, tok, 2 * units), BF16), shape_of((count, tok, units), BF16)]
    if last:
        in_specs.append(
            pl.BlockSpec((1, tile, width), lambda s, i, info: (info[0], leave(s, i), 0))
        )
        half = tok // tile // 2
        out_specs += [
            pl.BlockSpec(
                (tile, width), lambda s, i, info: (jnp.minimum(leave(s, i), half - 1), 0)
            ),
            pl.BlockSpec(
                (tile, width), lambda s, i, info: (jnp.maximum(leave(s, i) - half, 0), 0)
            ),
            tiles(width),
            tiles(width),
            pl.BlockSpec((width, tile), lambda s, i, info: (0, leave(s, i))),
            pl.BlockSpec((1, width // 4), lambda s, i, info: (0, 0)),
        ]
        out_shape += [
            shape_of((tok // 2, width), BF16),
            shape_of((tok // 2, width), BF16),
            shape_of((tok, width), F32),
            shape_of((tok, width), BF16),
            shape_of((width, tok), BF16),
            shape_of((1, width // 4), F32),
        ]
    else:
        out_specs.append(tiles(width))
        out_shape.append(shape_of((tok, width), F32))
    return pl.pallas_call(
        functools.partial(ffn_fwd_kernel, tile, [plan for plan, _ in weights], last),
        grid_spec=pltpu.PrefetchScalarGridSpec(
            num_scalar_prefetch=1,
            grid=(count, tok // tile),
            in_specs=in_specs + [ANY] * len(pieces),
            out_specs=out_specs,
            scratch_shapes=[
                pltpu.VMEM((count, width, 2 * units), BF16),
                pltpu.VMEM((count, width, units), BF16),
                pltpu.VMEM((tok, width), F32),
                pltpu.SemaphoreType.DMA((count, 2)),
            ],
        ),
        out_shape=out_shape,
        compiler_params=settings(2, 60),
        cost_estimate=cost(True),
        name="ffn_fwd",
    )(info, scale, x, total, *([teacher] if last else []), *pieces)


def ffn_bwd_kernel(steps, plan, first, low_ref, act_ref, hid_ref, xt_ref, lowt_ref, *rest):
    count = 1 + max(place[0] for chunks in plan for place in chunks)
    pieces, rest = rest[:count], rest[count:]
    if not first:
        in_ref, rest = rest[0], rest[1:]
    out_ref, keep_ref, send_ref, gate_up, down, dact_all, hid_all, sems = rest
    step = pl.program_id(0)
    units = down.shape[1]
    third = units // 3
    tile = low_ref.shape[0]

    @pl.when(step == 0)
    def _():
        wide, thin = weight_copies(plan, pieces, gate_up, down, sems.at[0], sems.at[1])
        for copy in thin + wide:
            copy.start()
        pltpu.make_async_copy(down, down, sems.at[1]).wait()

    @pl.when(step < steps)
    def _():
        rows = pl.ds(pl.multiple_of(step * tile, tile), tile)
        grad_hidden = dot(low_ref[...], down[...], 1, 0)
        for j, (to_gate, to_upper) in enumerate(split_act(act_ref[0])):
            grad = grad_hidden[:, j * third : (j + 1) * third]
            at = 2 * j * third
            dact_all[rows, at : at + third] = (grad * to_gate.astype(F32)).astype(BF16)
            dact_all[rows, at + third : at + 2 * third] = (grad * to_upper.astype(F32)).astype(BF16)
        hid_all[rows, :] = hid_ref[0]

        @pl.when(step == 0)
        def _():
            pltpu.make_async_copy(gate_up, gate_up, sems.at[0]).wait()

        grown = dot(dact_all[rows, :], gate_up[...], 1, 1)
        out_ref[...] = grown if first else in_ref[...] + grown

    def weight_rows(target):
        target[:, : 2 * units] = dot(xt_ref[...], dact_all[...], 1, 0).astype(BF16)
        target[:, 2 * units :] = dot(lowt_ref[...], hid_all[...], 1, 0).astype(BF16)

    @pl.when((step >= steps) & (step < steps + 2))
    def _():
        weight_rows(send_ref)

    @pl.when(step >= steps + 2)
    def _():
        weight_rows(keep_ref)


def ffn_bwd(low, saved, weights, total, xt, lowt, tile):
    plan, pieces = weights
    acts, hiddens, block = saved
    tok, width = low.shape
    units = hiddens.shape[2]
    steps = tok // tile
    quarter = width // 4
    first = total is None
    clip = lambda i: jnp.minimum(i, steps - 1)
    rows_of = lambda n: pl.BlockSpec((tile, n), lambda i: (clip(i), 0))
    slab = lambda n: pl.BlockSpec((1, tile, n), lambda i: (block, clip(i), 0))
    feature = lambda i: (jnp.where(i < steps + 2, jnp.maximum(i - steps, 0) + 2, i - steps - 2), 0)
    return pl.pallas_call(
        functools.partial(ffn_bwd_kernel, steps, plan, first),
        grid=(steps + 4,),
        in_specs=[
            rows_of(width),
            slab(2 * units),
            slab(units),
            pl.BlockSpec((quarter, tok), feature),
            pl.BlockSpec((quarter, tok), feature),
        ]
        + [ANY] * len(pieces)
        + ([] if first else [rows_of(width)]),
        out_specs=[
            rows_of(width),
            pl.BlockSpec((quarter, 3 * units), lambda i: (jnp.maximum(i - steps - 2, 0), 0)),
            pl.BlockSpec((quarter, 3 * units), lambda i: (jnp.clip(i - steps, 0, 1), 0)),
        ],
        out_shape=[
            shape_of((tok, width), F32),
            shape_of((width // 2, 3 * units), BF16),
            shape_of((width // 2, 3 * units), BF16),
        ],
        scratch_shapes=[
            pltpu.VMEM((width, 2 * units), BF16),
            pltpu.VMEM((width, units), BF16),
            pltpu.VMEM((tok, 2 * units), BF16),
            pltpu.VMEM((tok, units), BF16),
            pltpu.SemaphoreType.DMA((2,)),
        ],
        input_output_aliases={} if first else {5 + len(pieces): 0},
        compiler_params=settings(1, 60),
        cost_estimate=cost(True),
        name="ffn_bwd",
    )(low, acts, hiddens, xt, lowt, *pieces, *([] if first else [total]))


def turn_chunks(block):
    wide = block.shape[1] * 2 // 9
    thin = wide // 2
    starts = [(2 * wide, wide), (wide, wide), (0, wide)]
    starts += [(3 * wide + 2 * thin, thin), (3 * wide + thin, thin), (3 * wide, thin)]
    return jnp.concatenate([block[:, a : a + n] for a, n in starts], axis=1)


def sum_kernel(turns, *refs):
    total = None
    for ref, turn in zip(refs[:-1], turns):
        value = ref[...].astype(F32)
        value = turn_chunks(value) if turn else value
        total = value if total is None else total + value
    refs[-1][...] = total.astype(refs[-1].dtype)


def summed(terms, turns=None, dtype=BF16):
    rows, cols = terms[0].shape
    spec = pl.BlockSpec((128, cols), lambda i: (i, 0))
    return pl.pallas_call(
        functools.partial(sum_kernel, turns or [False] * len(terms)),
        grid=(rows // 128,),
        in_specs=[spec] * len(terms),
        out_specs=spec,
        out_shape=shape_of((rows, cols), dtype),
        compiler_params=settings(1, 60),
        cost_estimate=cost(False),
        name="summed",
    )(*terms)


def sums_kernel(jobs, count, info, *refs):
    arrays, refs = refs[:count], refs[count:]
    outs, (term_buf, out_buf, term_sems, out_sems) = refs[: len(jobs)], refs[len(jobs) :]
    rows = term_buf.shape[1]
    copies = []
    for terms in jobs:
        group = []
        for array, base, pick, _ in terms:
            at = base
            if pick is not None:
                at = pl.multiple_of(base + jnp.bitwise_xor(info[2], pick) * rows, rows)
            i = len(copies) + len(group)
            src = arrays[array].at[pl.ds(at, rows)]
            group.append(pltpu.make_async_copy(src, term_buf.at[i], term_sems.at[i]))
            group[-1].start()
        copies += group
    first = 0
    stores = []
    for j, terms in enumerate(jobs):
        total = None
        for i, (_, _, _, turn) in enumerate(terms):
            copies[first + i].wait()
            value = term_buf[first + i].astype(F32)
            value = turn_chunks(value) if turn else value
            total = value if total is None else total + value
        first += len(terms)
        out_buf[j] = total.astype(BF16)
        stores.append(pltpu.make_async_copy(out_buf.at[j], outs[j], out_sems.at[j]))
        stores[-1].start()
    for store in stores:
        store.wait()


def sums(info, arrays, jobs):
    cols = arrays[0].shape[1]
    rows, terms = 128, sum(len(job) for job in jobs)
    return pl.pallas_call(
        functools.partial(sums_kernel, jobs, len(arrays)),
        grid_spec=pltpu.PrefetchScalarGridSpec(
            num_scalar_prefetch=1,
            grid=(1,),
            in_specs=[ANY] * len(arrays),
            out_specs=[ANY] * len(jobs),
            scratch_shapes=[
                pltpu.VMEM((terms, rows, cols), BF16),
                pltpu.VMEM((len(jobs), rows, cols), BF16),
                pltpu.SemaphoreType.DMA((terms,)),
                pltpu.SemaphoreType.DMA((len(jobs),)),
            ],
        ),
        out_shape=[shape_of((rows, cols), BF16)] * len(jobs),
        compiler_params=settings(1, 60),
        cost_estimate=cost(False),
        name="sums",
    )(info, *arrays)


def core_jobs(keep, came):
    return [[(a, far * 256, pick, False) for a in (keep, came)] for far in (0, 1) for pick in (0, 1)]


def core_sum_kernel(info, left_ref, right_ref, *outs):
    total = (left_ref[...].astype(F32) + right_ref[...].astype(F32)).astype(BF16)
    block = pl.program_id(1)
    place = block // 2 * 2 + jnp.bitwise_xor(block % 2, info[2])
    for i, out in enumerate(outs):

        @pl.when(place == i)
        def _():
            out[...] = total


def core_sum(info, keep, came):
    groups, rows, cols = keep.shape
    spec = pl.BlockSpec((1, rows // 4, cols), lambda g, i, info: (g, i, 0))
    return pl.pallas_call(
        core_sum_kernel,
        grid_spec=pltpu.PrefetchScalarGridSpec(
            num_scalar_prefetch=1,
            grid=(groups, 4),
            in_specs=[spec] * 2,
            out_specs=[pl.BlockSpec((1, rows // 4, cols), lambda g, i, info: (g, 0, 0))] * 4,
        ),
        out_shape=[shape_of((groups, rows // 4, cols), BF16)] * 4,
        compiler_params=settings(2, 24),
        cost_estimate=cost(False),
        name="core_sum",
    )(info, keep, came)


def weight_grad_kernel(nt_ref, back0_ref, back1_ref, gt_ref, att_ref, keep_ref, send_ref):
    cols = back0_ref.shape[2]
    part, block = pl.program_id(0), pl.program_id(1)

    def rows(target, back_ref):
        target[0, :, :cols] = dot(nt_ref[...], back_ref[0], 1, 0).astype(BF16)
        target[0, :, cols:] = dot(gt_ref[...], att_ref[0], 1, 0).astype(BF16)

    for j, back_ref in enumerate((back0_ref, back1_ref)):

        @pl.when((part == 0) & (block % 2 == j))
        def _():
            rows(send_ref, back_ref)

        @pl.when((part == 1) & (block % 2 == j))
        def _():
            rows(keep_ref, back_ref)


def weight_grad(normed_t, backs, grad_t, attended):
    width, tok = normed_t.shape
    cols, feats = backs[0].shape[2], attended.shape[2]
    half = pl.BlockSpec((width // 2, tok), lambda p, k: (1 - p, 0))
    side = pl.BlockSpec((1, tok, cols), lambda p, k: (k // 2, 0, 0))
    shape = (1, width // 2, cols + feats)
    return pl.pallas_call(
        weight_grad_kernel,
        grid=(2, 4),
        in_specs=[half, side, side, half, pl.BlockSpec((1, tok, feats), lambda p, k: (k, 0, 0))],
        out_specs=[
            pl.BlockSpec(shape, lambda p, k: (jnp.where(p == 0, 0, k), 0, 0)),
            pl.BlockSpec(shape, lambda p, k: (jnp.where(p == 0, k, 3), 0, 0)),
        ],
        out_shape=[shape_of((4, width // 2, cols + feats), BF16)] * 2,
        compiler_params=settings(2, 60),
        cost_estimate=cost(True),
        name="weight_grad",
    )(normed_t, *backs, grad_t, attended)


def after(value, *others):
    return lax.optimization_barrier((value,) + others)[0]


def per_device_rows(
    tokens,
    teacher,
    lengths,
    attn_gain,
    q_weight,
    k_weight,
    v_weight,
    q_gain,
    k_gain,
    o_weight,
    ffn_gain,
    gate_weight,
    up_weight,
    down_weight,
):
    z = lax.axis_index("tp")
    ctx = lax.axis_index("ctx")
    fsdp = lax.axis_index("fsdp")
    rows_dev, tok, width = tokens.shape
    quarter = width // 4
    hd = q_gain.shape[0] * 4
    q_cols, k_cols = q_weight.shape[1], k_weight.shape[1]
    proj = q_cols + 2 * k_cols
    heads = (q_cols // hd, k_cols // hd)
    units = gate_weight.shape[1]
    slots = rows_dev * 4 * tok * 2

    def x_swap(v):
        return lax.ppermute(v, "fsdp", X_SWAP)

    def core_swap(v):
        return lax.ppermute(v, "fsdp", CORE_SWAP)

    def y_swap(v):
        return lax.ppermute(v, "ctx", Y_SWAP)

    def z_up(v):
        return lax.ppermute(v, "tp", Z_UP)

    def z_far(v):
        return lax.ppermute(v, "tp", Z_FAR)

    def z_down(v):
        return lax.ppermute(v, "tp", Z_DOWN)

    def natural(v):
        v = jnp.concatenate([v[0:1], v[2:3], v[1:2], v[3:4]], axis=0)
        v = jnp.where(fsdp % 2 == 0, v, jnp.concatenate([v[1:2], v[0:1], v[3:4], v[2:3]], axis=0))
        return jnp.where(fsdp // 2 == 0, v, jnp.concatenate([v[2:4], v[0:2]], axis=0))

    v = {}

    def sync():
        v.update(lax.optimization_barrier(dict(v)))

    length = lax.dynamic_slice_in_dim(lengths, z, 1, 0)
    info = jnp.concatenate([jnp.stack([z, fsdp, ctx]).astype(jnp.int32), length])
    w_proj = join(q_weight, k_weight, v_weight)
    proj_z = [z_up(w_proj), z_far(w_proj), z_down(w_proj)]
    proj_own = jnp.concatenate([w_proj, x_swap(w_proj)], axis=0)
    count_here = jnp.sum(lengths).astype(F32)[None]
    vector = jnp.concatenate([attn_gain, ffn_gain, q_gain, k_gain]).astype(F32)
    vector = jnp.concatenate([vector, count_here, jnp.zeros((640 - 545,), F32)])[None]
    vector = jnp.concatenate([vector, x_swap(vector)], axis=0)
    vector = jnp.concatenate([vector, core_swap(vector)], axis=0)
    w_out, w_ffn, *w_chunks = pack(info, o_weight, gate_weight, up_weight, down_weight)
    pos = (ctx * tok + jnp.arange(tok, dtype=jnp.int32)).astype(F32)
    frequency = THETA ** (-(2.0 * jnp.arange(hd // 2, dtype=F32)) / hd)
    angles = frequency[:, None] * pos[None, :]
    head_gains = natural(vector[:, 2 * quarter : 544])
    v.update(
        info=info,
        proj_own=proj_own,
        proj_z=jnp.concatenate(proj_z, axis=0),
        w_out=w_out,
        w_ffn=w_ffn,
        w_chunks=w_chunks,
        gain_one=vector[:, :quarter].reshape(1, width),
        gain_two=vector[:, quarter : 2 * quarter].reshape(1, width),
        total_count=jnp.sum(vector[:, 544]),
        gain_q=head_gains[:, : hd // 4].reshape(hd, 1),
        gain_k=head_gains[:, hd // 4 :].reshape(hd, 1),
        cos_part=jnp.cos(angles),
        sin_part=jnp.sin(angles),
    )
    sync()
    info = v["info"]

    proj_zfar = x_swap(v["proj_z"])
    out_z = [z_up(v["w_out"]), z_far(v["w_out"]), z_down(v["w_out"])]
    own_core = core_swap(v["proj_own"])
    x_in, normed_one_t = norm_one(info, tokens, v["gain_one"], 256)
    v.update(
        proj_zfar=proj_zfar, own_core=own_core, x_in=x_in, normed_one_t=normed_one_t, out_z=out_z
    )
    sync()

    plan_proj = [[(0, 0), (0, quarter), (3, 0), (3, quarter)]]
    plan_proj += [[(p, k * quarter) for p in (1, 2, 4, 5)] for k in range(3)]
    weights_proj = [v["proj_own"], v["proj_z"], v["proj_zfar"], v["own_core"]]
    weights_proj += [core_swap(v["proj_z"]), core_swap(v["proj_zfar"])]
    one = [z_up(v["w_chunks"][0]), z_up(v["w_chunks"][3])]
    ffn_far = x_swap(v["w_ffn"])
    tables = [v[name] for name in ("cos_part", "sin_part", "gain_q", "gain_k")]

    def make(block, *then):
        normed_t = after(v["normed_one_t"], *then)
        return project(info, (plan_proj, weights_proj), normed_t, *tables, heads, block)

    theirs = [make(lambda s: 2 * (1 - s[2]))]
    got = [y_swap(theirs[0][0])]
    theirs.append(make(lambda s: 2 * (1 - s[2]) + 1, theirs[0][0]))
    got.append(y_swap(theirs[1][0]))
    mine = [make(lambda s: 2 * s[2], theirs[1][0])]
    mine.append(make(lambda s: 2 * s[2] + 1, mine[0][0]))
    v.update(
        one=one,
        ffn_far=ffn_far,
        weights_proj=weights_proj,
        mine=mine,
        theirs=theirs,
        got0=got[0],
    )
    sync()

    one_far = [x_swap(v["one"][0])]
    three = [z_down(v["w_chunks"][0])]
    own_cores = [core_swap(v["w_ffn"]), core_swap(v["ffn_far"])]
    first = attn_fwd(info, v["mine"][0][0], v["got0"], hd)
    v.update(first=first, got1=got[1], one_far=one_far, three=three, own_cores=own_cores)
    sync()

    arrived = [y_swap(v["first"][1])]
    three = v["three"] + [z_down(v["w_chunks"][1])]
    out_blocks = jnp.concatenate([v["w_out"]] + v["out_z"], axis=0)
    out_far = x_swap(out_blocks)
    one_cores = [core_swap(v["one"][0]), core_swap(v["one_far"][0])]
    second = attn_fwd(info, v["mine"][1][0], v["got1"], hd)
    v.update(
        second=second,
        arrived=arrived,
        three=three,
        out_blocks=out_blocks,
        out_far=out_far,
        one_cores=one_cores,
    )
    sync()

    arrived = v["arrived"] + [y_swap(v["second"][1])]
    three = v["three"] + [z_down(v["w_chunks"][2])]
    one_far = v["one_far"] + [x_swap(v["one"][1][:, :units])]
    weights_out = [v["out_blocks"], v["out_far"]]
    weights_out += [core_swap(v["out_blocks"]), core_swap(v["out_far"])]
    v.update(arrived=arrived, three=three, one_far=one_far, weights_out=weights_out)
    sync()

    plan_out = [[(p, k * quarter) for p in range(4)] for k in range(4)]
    two = [z_up(v["one"][0])]
    three_far = [x_swap(v["three"][0])]
    one_far = v["one_far"] + [y_swap(v["one_far"][0])]
    one_cores = v["one_cores"] + [core_swap(v["one"][1]), core_swap(v["one_far"][1])]
    resid, normed_two, normed_two_t, attended = out_proj(
        info,
        v["x_in"],
        [v["first"][0], v["second"][0]],
        v["arrived"],
        (plan_out, v["weights_out"]),
        v["gain_two"],
        256,
    )
    v.update(
        two=two,
        three_far=three_far,
        one_far=one_far,
        one_cores=one_cores,
        resid=resid,
        normed_two=normed_two,
        normed_two_t=normed_two_t,
        attended=attended,
    )
    sync()

    plan0 = [[(i, 0, j * units) for j in range(3)] for i in range(4)]
    plan_mixed = [[(0, 0, 0), (1, 0, 0), (1, 0, units)], [(i, 0, 0) for i in (2, 3, 4)]]
    plan_mixed += [[(5, 0, 0), (6, 0, 0), (6, 0, units)], [(i, 0, 0) for i in (7, 8, 9)]]
    scale = (slots / v["total_count"])[None]
    weights0 = [v["w_ffn"], v["ffn_far"]] + v["own_cores"]
    c0, cf, c1, cb = v["one_cores"]
    weights1 = v["one"] + v["one_far"] + [c0, c1, cf, cb, core_swap(v["one_far"][2])]
    two = v["two"] + [z_up(v["one"][1])]
    three_far = v["three_far"] + [x_swap(v["three"][1]), y_swap(v["three_far"][0])]
    two_far = [x_swap(v["two"][0])]
    three_cores = [core_swap(v["three"][0])]
    acts_a, hiddens_a, sum_a = ffn_fwd(
        info,
        scale,
        v["normed_two"],
        v["resid"],
        None,
        [(plan0, weights0), (plan_mixed, weights1)],
        units,
        256,
    )
    v.update(
        scale=scale,
        weights0=weights0,
        weights1=weights1,
        two=two,
        three_far=three_far,
        two_far=two_far,
        three_cores=three_cores,
        acts_a=acts_a,
        hiddens_a=hiddens_a,
        sum_a=sum_a,
    )
    sync()

    plan_chunks = [[(3 * p + j, 0, 0) for j in range(3)] for p in range(4)]
    weights3 = v["three"] + v["three_far"] + v["three_cores"]
    weights3 += [core_swap(part) for part in v["three"][1:]]
    weights3 += [core_swap(part) for part in v["three_far"]]
    two_far = v["two_far"] + [x_swap(v["two"][1][:, :units]), y_swap(v["two_far"][0])]
    two_cores = [core_swap(part) for part in v["two"] + v["two_far"]]
    acts_b, hiddens_b, sum_b = ffn_fwd(
        info, v["scale"], v["normed_two"], v["sum_a"], None, [(plan_chunks, weights3)], units, 256
    )
    v.update(
        weights3=weights3,
        two_far=two_far,
        two_cores=two_cores,
        acts_b=acts_b,
        hiddens_b=hiddens_b,
        sum_b=sum_b,
    )
    sync()

    weights2 = v["two"] + v["two_far"] + v["two_cores"]
    weights2 += [core_swap(part) for part in v["two_far"][1:]]
    acts_c, hiddens_c, *results, grad_result, grad_low, grad_low_t, square = ffn_fwd(
        info, v["scale"], v["normed_two"], v["sum_b"], teacher, [(plan_mixed, weights2)], units, 256
    )
    v.update(
        weights2=weights2,
        acts_c=acts_c,
        hiddens_c=hiddens_c,
        results=results,
        grad_result=grad_result,
        grad_low=grad_low,
        grad_low_t=grad_low_t,
        square=square,
    )
    sync()

    def ffn_back(plan, weights, acts, hiddens, block, total):
        return ffn_bwd(
            v["grad_low"],
            (v[acts], v[hiddens], block),
            (plan, v[weights]),
            total,
            v["normed_two_t"],
            v["grad_low_t"],
            256,
        )

    turned = [False, False, True]
    one = [z_up(v["results"][0])]
    total, keep2, send2 = ffn_back(plan_mixed, "weights2", "acts_c", "hiddens_c", 0, None)
    v.update(one=one, total=total, keep2=keep2, send2=send2)
    sync()

    one = v["one"] + [z_up(v["results"][1])]
    came2 = core_swap(v["send2"])
    total, keep1, send1 = ffn_back(plan_mixed, "weights1", "acts_a", "hiddens_a", 1, v["total"])
    v.update(one=one, came2=came2, total=total, keep1=keep1, send1=send1)
    sync()

    out_three = [z_down(v["results"][0])]
    came1 = core_swap(v["send1"])
    sum2 = sums(info, [v["keep2"], v["came2"]], core_jobs(0, 1))
    far_t2 = x_swap(sum2[3])
    total, keep3, send3 = ffn_back(
        plan_chunks, "weights3", "acts_b", "hiddens_b", 0, after(v["total"], sum2[0])
    )
    v.update(
        out_three=out_three,
        came1=came1,
        sum2=sum2,
        far_t2=far_t2,
        total=total,
        keep3=keep3,
        send3=send3,
    )
    sync()

    out_three = v["out_three"] + [z_down(v["results"][1])]
    came3 = core_swap(v["send3"])
    far_h2 = x_swap(v["sum2"][2])
    there2, *sum1 = sums(
        info,
        [v["sum2"][1], v["far_t2"], v["keep1"], v["came1"]],
        [[(0, 0, None, False), (1, 0, None, False)]] + core_jobs(2, 3),
    )
    there2 = y_swap(there2)
    total, keep0, send0 = ffn_back(
        plan0, "weights0", "acts_a", "hiddens_a", 0, after(v["total"], sum1[0])
    )
    v.update(
        out_three=out_three,
        came3=came3,
        far_h2=far_h2,
        there2=there2,
        sum1=sum1,
        total=total,
        keep0=keep0,
        send0=send0,
    )
    sync()

    came0 = core_swap(v["send0"])
    far_t1 = x_swap(v["sum1"][3])
    plane = [(0, 0, None, False), (1, 0, None, False), (2, 0, None, True)]
    part2, *sum3 = sums(
        info,
        [v["sum2"][0], v["far_h2"], v["there2"], v["keep3"], v["came3"]],
        [plane] + core_jobs(3, 4),
    )
    down2 = z_down(part2)
    grad_resid, grad_attn_t, a0, a1, b0, b1, gain_two_sum = norm_two_back(
        info,
        after(v["total"], sum3[0]),
        v["resid"],
        v["grad_result"],
        v["gain_two"],
        (plan_out, v["weights_out"]),
        256,
    )
    grad_got = [y_swap(b0), y_swap(b1)]
    v.update(
        came0=came0,
        far_t1=far_t1,
        down2=down2,
        sum3=sum3,
        grad_resid=grad_resid,
        grad_attn_t=grad_attn_t,
        grad_mine=[a0, a1],
        gain_two_sum=gain_two_sum,
        grad_got0=grad_got[0],
    )
    sync()

    def attn_back(j, grad):
        out, got_ref = v["first" if j == 0 else "second"], v[f"got{j}"]
        return attn_bwd(
            info, v["mine"][j][0], got_ref, out[0], out[1], grad, v[f"grad_got{j}"], out[2], hd
        )

    two = [z_up(v["one"][0])]
    far_h1 = x_swap(v["sum1"][2])
    there1, *sum0 = sums(
        info,
        [v["sum1"][1], v["far_t1"], v["keep0"], v["came0"]],
        [[(0, 0, None, False), (1, 0, None, False)]] + core_jobs(2, 3),
    )
    there1 = y_swap(there1)
    far_t3 = x_swap(v["sum3"][3])
    back0 = attn_back(0, after(v["grad_mine"][0], sum0[0]))
    v.update(
        out_two=two,
        far_h1=far_h1,
        there1=there1,
        far_t3=far_t3,
        sum0=sum0,
        back0=back0,
        grad_got1=grad_got[1],
    )
    sync()

    two = v["out_two"] + [z_up(v["one"][1])]
    heads0 = y_swap(v["back0"][1])
    far_h3 = x_swap(v["sum3"][2])
    far_t0 = x_swap(v["sum0"][3])
    there3, two_down = sums(
        info,
        [v["sum3"][1], v["far_t3"], v["sum1"][0], v["far_h1"], v["there1"], v["down2"]],
        [
            [(0, 0, None, False), (1, 0, None, False)],
            [(2, 0, None, False), (3, 0, None, False), (4, 0, None, True), (5, 0, None, False)],
        ],
    )
    there3_got = y_swap(there3)
    two_down_got = z_down(two_down)
    back1 = attn_back(1, after(v["grad_mine"][1], there3, two_down))
    v.update(
        out_two=two, heads0=heads0, far_h3=far_h3, far_t0=far_t0, there3=there3_got, back1=back1
    )
    sync()

    heads1 = y_swap(v["back1"][1])
    far_h0 = x_swap(v["sum0"][2])
    part3, there0 = sums(
        info,
        [v["sum3"][0], v["far_h3"], v["there3"], v["sum0"][1], v["far_t0"]],
        [plane, [(3, 0, None, False), (4, 0, None, False)]],
    )
    up3 = z_up(part3)
    tables = [v[name] for name in ("cos_part", "sin_part", "gain_q", "gain_k")]
    head0 = head_back(
        info, v["back0"][0], v["heads0"], v["mine"][0][1], v["theirs"][0][1], *tables, heads
    )
    v.update(heads1=heads1, head0=head0, there0=there0)
    sync()

    there0 = y_swap(v["there0"])
    head1 = head_back(
        info, v["back1"][0], v["heads1"], v["mine"][1][1], v["theirs"][1][1], *tables, heads
    )
    def last_norm(part, *then):
        return norm_one_back(
            info,
            [v["head0"][0], after(head1[0], *then)],
            (plan_proj, v["weights_proj"]),
            v["x_in"],
            v["grad_resid"],
            v["gain_one"],
            tok // 4,
            part,
        )

    low_first, gain_first = last_norm(0)
    low_second, gain_second = last_norm(1, low_first)
    gathered = [lax.all_gather(low_first, "tp", axis=0, tiled=False)]
    tokens_low, gain_one_sum = low_second, gain_first + gain_second
    v.update(head1=head1, tokens_low=tokens_low, gain_one_sum=gain_one_sum, up3=up3)
    v.update(there0=there0, far_h0=far_h0, two_down=two_down_got)
    sync()

    def place(out, parts, k, first):
        row = lax.rem(z - k + 4, 4)
        for j, part in enumerate(parts):
            at = (first + j) * part.shape[0]
            out = lax.dynamic_update_slice(out, part.astype(out.dtype)[None], (row, at, 0))
        return out

    v.update(out_one=v["one"])
    gathered.append(lax.all_gather(v["tokens_low"], "tp", axis=0, tiled=False))
    keep, send = weight_grad(
        v["normed_one_t"], [v["head0"][0], v["head1"][0]], v["grad_attn_t"], v["attended"]
    )
    gain_heads = v["head0"][1] + v["head1"][1]
    vector = jnp.concatenate(
        [
            natural(v["gain_one_sum"].reshape(4, quarter)).reshape(1, width),
            natural(v["gain_two_sum"].reshape(4, quarter)).reshape(1, width),
            gain_heads[:, 0].reshape(1, hd),
            gain_heads[:, 1].reshape(1, hd),
            jnp.sum(v["square"]).reshape(1, 1),
            jnp.zeros((1, 127), F32),
        ],
        axis=1,
    )
    vector = vector + core_swap(vector)
    v.update(keep=keep, send=send)
    v.update(vector=vector)
    sync()

    rows = quarter // 2
    flat = lambda a: a.reshape(4 * rows, a.shape[-1])
    attn_sums = [flat(p) for p in core_sum(info, v["keep"], core_swap(v["send"]))]
    vector = v["vector"] + x_swap(v["vector"])
    v.update(sums=attn_sums, vector=vector)
    sync()

    far_t = x_swap(v["sums"][3])
    part0 = summed([v["sum0"][0], v["far_h0"], v["there0"]], turned)
    ffn_sum = summed([part0, v["two_down"], v["up3"]], None, F32)
    vector = v["vector"] + y_swap(v["vector"])
    v.update(far_t=far_t, ffn_sum=ffn_sum, vector=vector)
    sync()

    far_h = x_swap(v["sums"][2])
    there = y_swap(summed([v["sums"][1], v["far_t"]]))
    output = jnp.zeros((rows_dev, tok, width), BF16)
    for k, parts in enumerate((v["results"], v["out_one"], v["out_two"], v["out_three"])):
        output = place(output, parts, k, 0)
    v.update(far_h=far_h, there=there, output=output)
    sync()

    parts = summed([v["sums"][0], v["far_h"], v["there"]])
    parts = [parts[k * rows : (k + 1) * rows] for k in range(4)]
    parts = [parts[0], z_down(parts[1]), z_far(parts[2]), z_up(parts[3])]
    ffn_other = y_swap(v["ffn_sum"])
    v.update(parts=parts)
    sync()

    attn_sum = summed(v["parts"], None, F32)
    vector = v["vector"] + lax.ppermute(v["vector"], "tp", Z_NEAR)
    v.update(attn_sum=attn_sum, vector=vector)
    v.update(ffn_other=ffn_other)
    sync()

    def finish(own, other):
        return jnp.concatenate(
            [jnp.where(ctx == 0, own, other), jnp.where(ctx == 0, other, own)], axis=0
        )

    def columns(first):
        parts = [ffn_grad[:, first(j) : first(j) + third] for j in range(3)]
        return jnp.concatenate(
            [
                jnp.where(ctx == 0, parts[0], parts[2]),
                parts[1],
                jnp.where(ctx == 0, parts[2], parts[0]),
            ],
            axis=1,
        )

    attn_other = y_swap(v["attn_sum"])
    vector = v["vector"] + lax.ppermute(v["vector"], "tp", Z_FAR)
    third = units // 3
    ffn_grad = finish(v["ffn_sum"], turn_chunks(v["ffn_other"]))
    grad_gate = columns(lambda j: 2 * j * third)
    grad_up = columns(lambda j: (2 * j + 1) * third)
    grad_down = columns(lambda j: 2 * units + j * third).T
    grad = jnp.zeros((rows_dev, tok, width), F32)
    grad = lax.dynamic_update_slice(grad, gathered[0].astype(F32), (0, 0, 0))
    v.update(vector=vector, attn_other=attn_other, grad=grad)
    v.update(grad_gate=grad_gate, grad_up=grad_up, grad_down=grad_down)
    sync()

    tokens_grad = lax.dynamic_update_slice(v["grad"], gathered[1].astype(F32), (0, tok // 2, 0))
    output = v["output"]
    sums_all = v["vector"][0]

    attn_grad = finish(v["attn_sum"], v["attn_other"])
    teacher_loss = sums_all[2 * width + 2 * hd] / (v["total_count"] * width)

    def own_part(at, size):
        return lax.dynamic_slice_in_dim(sums_all, at + fsdp * (size // 4), size // 4, 0)

    return (
        output,
        teacher_loss,
        tokens_grad,
        own_part(0, width),
        attn_grad[:, :q_cols],
        attn_grad[:, q_cols : q_cols + k_cols],
        attn_grad[:, q_cols + k_cols : proj],
        own_part(2 * width, hd),
        own_part(2 * width + hd, hd),
        attn_grad[:, proj:].T,
        own_part(width, width),
        v["grad_gate"],
        v["grad_up"],
        v["grad_down"],
    )


def solution(mesh):
    return jax.shard_map(
        per_device_rows if fits(mesh) else per_device_any,
        mesh=mesh,
        in_specs=(
            P("fsdp", "ctx", None),
            P("fsdp", "ctx", None),
            P("fsdp"),
            P("fsdp"),
            P("fsdp", "tp"),
            P("fsdp", "tp"),
            P("fsdp", "tp"),
            P("fsdp"),
            P("fsdp"),
            P("tp", "fsdp"),
            P("fsdp"),
            P("fsdp", "tp"),
            P("fsdp", "tp"),
            P("tp", "fsdp"),
        ),
        out_specs=(
            P("fsdp", "ctx", None),
            P(),
            P("fsdp", "ctx", None),
            P("fsdp"),
            P("fsdp", "tp"),
            P("fsdp", "tp"),
            P("fsdp", "tp"),
            P("fsdp"),
            P("fsdp"),
            P("tp", "fsdp"),
            P("fsdp"),
            P("fsdp", "tp"),
            P("fsdp", "tp"),
            P("tp", "fsdp"),
        ),
        check_vma=False,
    )
```

```python
import functools
import math

import jax
import jax.numpy as jnp
from jax import lax
from jax.experimental import pallas as pl
from jax.experimental.pallas import tpu as pltpu
from jax.sharding import PartitionSpec as P

EPS = 1e-05
THETA = 1000000.0
NEGATIVE = -1e30


def rms_scale(field_in, gain_vec):
    return (
        field_in * lax.rsqrt(jnp.mean(field_in * field_in, axis=-1, keepdims=True) + EPS) * gain_vec
    )


def rotate(field_in, positions):
    half_dim = field_in.shape[-1] // 2
    frequency = THETA ** (-(2.0 * jnp.arange(half_dim, dtype=jnp.float32)) / field_in.shape[-1])
    angles = positions[:, None] * frequency[None, :]
    cos_part = jnp.cos(angles)[:, None, :]
    sin_part = jnp.sin(angles)[:, None, :]
    lower_half = field_in[..., :half_dim]
    upper_half = field_in[..., half_dim:]
    return jnp.concatenate(
        [
            lower_half * cos_part - upper_half * sin_part,
            upper_half * cos_part + lower_half * sin_part,
        ],
        axis=-1,
    )


def linear(left_mat, right_mat):
    return jnp.dot(left_mat, right_mat, preferred_element_type=jnp.float32)


def linear_left(left_mat, right_mat):
    return lax.dot_general(
        left_mat, right_mat, (((0,), (0,)), ((), ())), preferred_element_type=jnp.float32
    )


def linear_right(left_mat, right_mat):
    return lax.dot_general(
        left_mat, right_mat, (((1,), (1,)), ((), ())), preferred_element_type=jnp.float32
    )


def swiglu(gate_act, up_act):
    return jax.nn.silu(gate_act) * up_act


def per_device_any(
    tokens,
    teacher,
    lengths,
    attn_gain,
    q_weight,
    k_weight,
    v_weight,
    q_gain,
    k_gain,
    o_weight,
    ffn_gain,
    gate_weight,
    up_weight,
    down_weight,
):
    (
        gain_one,
        w_query,
        w_key,
        w_value,
        gain_query,
        gain_key,
        w_output,
        gain_two,
        w_gate,
        w_upper,
        w_down,
    ) = (
        lax.all_gather(attn_gain, "fsdp", axis=0, tiled=True),
        lax.all_gather(q_weight, "fsdp", axis=0, tiled=True),
        lax.all_gather(k_weight, "fsdp", axis=0, tiled=True),
        lax.all_gather(v_weight, "fsdp", axis=0, tiled=True),
        lax.all_gather(q_gain, "fsdp", axis=0, tiled=True),
        lax.all_gather(k_gain, "fsdp", axis=0, tiled=True),
        lax.all_gather(o_weight, "fsdp", axis=1, tiled=True),
        lax.all_gather(ffn_gain, "fsdp", axis=0, tiled=True),
        lax.all_gather(gate_weight, "fsdp", axis=0, tiled=True),
        lax.all_gather(up_weight, "fsdp", axis=0, tiled=True),
        lax.all_gather(down_weight, "fsdp", axis=1, tiled=True),
    )
    rows_dev, block_len, model_width = tokens.shape
    count_tok = rows_dev * block_len
    head_dim = gain_query.shape[0]
    q_heads = w_query.shape[1] // head_dim
    kv_heads = w_key.shape[1] // head_dim
    group_size = q_heads // kv_heads
    score_scale = head_dim ** (-0.5)
    row_len = block_len * lax.axis_size("ctx")
    key_block = math.gcd(row_len, 512)
    block_start = lax.axis_index("ctx") * block_len
    tiles_used = (block_start + block_len + key_block - 1) // key_block
    slot_pos = block_start + jnp.arange(block_len, dtype=jnp.int32)
    positions = slot_pos.astype(jnp.float32)
    valid = (slot_pos[None, :] < lengths[:, None]).astype(jnp.float32)
    slots = count_tok * lax.axis_size("fsdp") * lax.axis_size("ctx")
    gain_two_f = gain_two.astype(jnp.float32)
    gain_one_f = gain_one.astype(jnp.float32)
    inputs = tokens.astype(jnp.float32)
    normed_one, back_one = jax.vjp(rms_scale, inputs, gain_one_f)
    normed_low = normed_one.astype(jnp.bfloat16).reshape(count_tok, model_width)
    query_raw = linear(normed_low, w_query)
    key_raw = linear(normed_low, w_key)
    value_raw = linear(normed_low, w_value)

    def heads_post(raw_heads, gain_vec):
        shaped = raw_heads.reshape(rows_dev, block_len, -1, head_dim)
        return rotate(rms_scale(shaped, gain_vec), positions)

    query_rot, query_back = jax.vjp(heads_post, query_raw, gain_query.astype(jnp.float32))
    key_rot, key_back = jax.vjp(heads_post, key_raw, gain_key.astype(jnp.float32))
    queries = query_rot.astype(jnp.bfloat16).reshape(
        rows_dev, block_len, kv_heads, group_size, head_dim
    )
    key_rows = key_rot.astype(jnp.bfloat16).reshape(rows_dev, block_len, kv_heads * head_dim)
    values = value_raw.astype(jnp.bfloat16).reshape(rows_dev, block_len, kv_heads * head_dim)
    keys_all, values_all = (
        lax.all_gather(key_rows, "ctx", axis=1, tiled=True),
        lax.all_gather(values, "ctx", axis=1, tiled=True),
    )

    def key_tile(tile_index):
        tile_start = tile_index * key_block
        key_pos = tile_start + jnp.arange(key_block, dtype=jnp.int32)
        key_part = lax.dynamic_slice_in_dim(keys_all, tile_start, key_block, 1).reshape(
            rows_dev, key_block, kv_heads, head_dim
        )
        value_part = lax.dynamic_slice_in_dim(values_all, tile_start, key_block, 1).reshape(
            rows_dev, key_block, kv_heads, head_dim
        )
        scores = (
            jnp.einsum("rqhgd,rkhd->rhgqk", queries, key_part, preferred_element_type=jnp.float32)
            * score_scale
        )
        allowed = (key_pos[None, None, :] <= slot_pos[None, :, None]) & (
            key_pos[None, None, :] < lengths[:, None, None]
        )
        return (tile_start, scores, allowed[:, None, None], key_part, value_part)

    stat_shape = (rows_dev, kv_heads, group_size, block_len)

    def stats_step(tile_index, carried):
        running_max, running_sum = carried
        tile_start, scores, allowed, key_part, value_part = key_tile(tile_index)
        masked = jnp.where(allowed, scores, NEGATIVE)
        new_max = jnp.maximum(running_max, jnp.max(masked, axis=-1))
        terms = jnp.where(allowed, jnp.exp(masked - new_max[..., None]), 0.0)
        return (new_max, running_sum * jnp.exp(running_max - new_max) + jnp.sum(terms, axis=-1))

    running_max, running_sum = lax.fori_loop(
        0,
        tiles_used,
        stats_step,
        (jnp.full(stat_shape, NEGATIVE, jnp.float32), jnp.zeros(stat_shape, jnp.float32)),
    )
    log_total = running_max + jnp.log(running_sum)
    out_shape = (rows_dev, block_len, kv_heads, group_size, head_dim)

    def value_step(tile_index, carried):
        rounded_out, exact_out = carried
        tile_start, scores, allowed, key_part, value_part = key_tile(tile_index)
        tile_probs = jnp.where(allowed, jnp.exp(scores - log_total[..., None]), 0.0)
        rounded_out = rounded_out + jnp.einsum(
            "rhgqk,rkhd->rqhgd",
            tile_probs.astype(jnp.bfloat16),
            value_part,
            preferred_element_type=jnp.float32,
        )
        exact_out = exact_out + jnp.einsum(
            "rhgqk,rkhd->rqhgd", tile_probs, value_part.astype(jnp.float32)
        )
        return (rounded_out, exact_out)

    rounded_out, exact_out = lax.fori_loop(
        0,
        tiles_used,
        value_step,
        (jnp.zeros(out_shape, jnp.float32), jnp.zeros(out_shape, jnp.float32)),
    )
    attended = rounded_out.astype(jnp.bfloat16).reshape(count_tok, q_heads * head_dim)
    attn_total = lax.psum(linear(attended, w_output), "tp")
    resid = inputs + attn_total.reshape(rows_dev, block_len, model_width)
    normed_two, back_two = jax.vjp(rms_scale, resid, gain_two_f)
    normed_second = normed_two.astype(jnp.bfloat16).reshape(count_tok, model_width)
    gate_act = linear(normed_second, w_gate)
    up_act = linear(normed_second, w_upper)
    hidden_full, back_glu = jax.vjp(swiglu, gate_act, up_act)
    hidden = hidden_full.astype(jnp.bfloat16)
    ffn_total = lax.psum(linear(hidden, w_down), "tp")
    result = resid + ffn_total.reshape(rows_dev, block_len, model_width)
    error_value = result - teacher.astype(jnp.float32)
    valid_col = valid[..., None]
    total_square, total_count = lax.psum(
        (jnp.sum(valid_col * error_value * error_value), jnp.sum(valid)), ("fsdp", "ctx")
    )
    teacher_loss = total_square / (total_count * model_width)
    grad_result = valid_col * error_value * (slots / total_count)
    grad_low = grad_result.astype(jnp.bfloat16).reshape(count_tok, model_width)
    grad_down = linear_left(hidden, grad_low)
    grad_hidden = linear_right(grad_low, w_down)
    grad_gate_full, grad_up_full = back_glu(grad_hidden)
    grad_gate = grad_gate_full.astype(jnp.bfloat16)
    grad_up = grad_up_full.astype(jnp.bfloat16)
    grad_wgate = linear_left(normed_second, grad_gate)
    grad_wup = linear_left(normed_second, grad_up)
    normed_two_part = linear_right(grad_gate, w_gate) + linear_right(grad_up, w_upper)
    grad_normed_two = lax.psum(normed_two_part, "tp")
    grad_resid_norm, grad_gain_two = back_two(
        grad_normed_two.reshape(rows_dev, block_len, model_width)
    )
    grad_resid = grad_result + grad_resid_norm
    grad_attn_low = grad_resid.astype(jnp.bfloat16).reshape(count_tok, model_width)
    grad_woutput = linear_left(attended, grad_attn_low)
    grad_attended = linear_right(grad_attn_low, w_output).astype(jnp.bfloat16).reshape(out_shape)
    delta = jnp.einsum("rqhgd,rqhgd->rhgq", grad_attended.astype(jnp.float32), exact_out)
    full_shape = (rows_dev, row_len, kv_heads * head_dim)

    def grad_step(tile_index, carried):
        grad_queries, grad_keys, grad_values = carried
        tile_start, scores, allowed, key_part, value_part = key_tile(tile_index)
        tile_probs = jnp.where(allowed, jnp.exp(scores - log_total[..., None]), 0.0)
        grad_probs = jnp.einsum(
            "rqhgd,rkhd->rhgqk", grad_attended, value_part, preferred_element_type=jnp.float32
        )
        grad_scores = (tile_probs * (grad_probs - delta[..., None])).astype(jnp.bfloat16)
        grad_queries = (
            grad_queries
            + jnp.einsum(
                "rhgqk,rkhd->rqhgd", grad_scores, key_part, preferred_element_type=jnp.float32
            )
            * score_scale
        )
        key_term = (
            jnp.einsum(
                "rhgqk,rqhgd->rkhd", grad_scores, queries, preferred_element_type=jnp.float32
            )
            * score_scale
        )
        value_term = jnp.einsum(
            "rhgqk,rqhgd->rkhd",
            tile_probs.astype(jnp.bfloat16),
            grad_attended,
            preferred_element_type=jnp.float32,
        )
        grad_keys = lax.dynamic_update_slice_in_dim(
            grad_keys, key_term.reshape(rows_dev, key_block, kv_heads * head_dim), tile_start, 1
        )
        grad_values = lax.dynamic_update_slice_in_dim(
            grad_values, value_term.reshape(rows_dev, key_block, kv_heads * head_dim), tile_start, 1
        )
        return (grad_queries, grad_keys, grad_values)

    grad_queries, grad_keys, grad_values = lax.fori_loop(
        0,
        tiles_used,
        grad_step,
        (
            jnp.zeros(out_shape, jnp.float32),
            jnp.zeros(full_shape, jnp.float32),
            jnp.zeros(full_shape, jnp.float32),
        ),
    )
    key_grad, value_grad = (
        lax.psum_scatter(grad_keys, "ctx", scatter_dimension=1, tiled=True),
        lax.psum_scatter(grad_values, "ctx", scatter_dimension=1, tiled=True),
    )
    grad_query_raw, grad_gain_query = query_back(
        grad_queries.reshape(rows_dev, block_len, q_heads, head_dim)
    )
    grad_key_raw, grad_gain_key = key_back(
        key_grad.reshape(rows_dev, block_len, kv_heads, head_dim)
    )
    query_low = grad_query_raw.astype(jnp.bfloat16)
    key_low = grad_key_raw.astype(jnp.bfloat16)
    value_low = value_grad.reshape(count_tok, kv_heads * head_dim).astype(jnp.bfloat16)
    grad_wquery = linear_left(normed_low, query_low)
    grad_wkey = linear_left(normed_low, key_low)
    grad_wvalue = linear_left(normed_low, value_low)
    normed_part = (
        linear_right(query_low, w_query)
        + linear_right(key_low, w_key)
        + linear_right(value_low, w_value)
    )
    grad_normed_one, grad_gain_query, grad_gain_key = lax.psum(
        (normed_part, grad_gain_query, grad_gain_key), "tp"
    )
    grad_input_norm, grad_gain_one = back_one(
        grad_normed_one.reshape(rows_dev, block_len, model_width)
    )
    tokens_grad = grad_resid + grad_input_norm
    partials = (
        grad_gain_one,
        grad_wquery,
        grad_wkey,
        grad_wvalue,
        grad_gain_query,
        grad_gain_key,
        grad_woutput,
        grad_gain_two,
        grad_wgate,
        grad_wup,
        grad_down,
    )
    pieces = (
        lax.psum_scatter(partials[0], ("fsdp", "ctx"), scatter_dimension=0, tiled=True),
        lax.psum_scatter(partials[1], ("fsdp", "ctx"), scatter_dimension=0, tiled=True),
        lax.psum_scatter(partials[2], ("fsdp", "ctx"), scatter_dimension=0, tiled=True),
        lax.psum_scatter(partials[3], ("fsdp", "ctx"), scatter_dimension=0, tiled=True),
        lax.psum_scatter(partials[4], ("fsdp", "ctx"), scatter_dimension=0, tiled=True),
        lax.psum_scatter(partials[5], ("fsdp", "ctx"), scatter_dimension=0, tiled=True),
        lax.psum_scatter(partials[6], ("fsdp", "ctx"), scatter_dimension=1, tiled=True),
        lax.psum_scatter(partials[7], ("fsdp", "ctx"), scatter_dimension=0, tiled=True),
        lax.psum_scatter(partials[8], ("fsdp", "ctx"), scatter_dimension=0, tiled=True),
        lax.psum_scatter(partials[9], ("fsdp", "ctx"), scatter_dimension=0, tiled=True),
        lax.psum_scatter(partials[10], ("fsdp", "ctx"), scatter_dimension=1, tiled=True),
    )
    summed = (
        lax.all_gather(pieces[0], "ctx", axis=0, tiled=True),
        lax.all_gather(pieces[1], "ctx", axis=0, tiled=True),
        lax.all_gather(pieces[2], "ctx", axis=0, tiled=True),
        lax.all_gather(pieces[3], "ctx", axis=0, tiled=True),
        lax.all_gather(pieces[4], "ctx", axis=0, tiled=True),
        lax.all_gather(pieces[5], "ctx", axis=0, tiled=True),
        lax.all_gather(pieces[6], "ctx", axis=1, tiled=True),
        lax.all_gather(pieces[7], "ctx", axis=0, tiled=True),
        lax.all_gather(pieces[8], "ctx", axis=0, tiled=True),
        lax.all_gather(pieces[9], "ctx", axis=0, tiled=True),
        lax.all_gather(pieces[10], "ctx", axis=1, tiled=True),
    )
    return (
        result.astype(jnp.bfloat16),
        teacher_loss,
        tokens_grad,
        summed[0],
        summed[1],
        summed[2],
        summed[3],
        summed[4],
        summed[5],
        summed[6],
        summed[7],
        summed[8],
        summed[9],
        summed[10],
    )


BF16 = jnp.bfloat16
F32 = jnp.float32
LOG2E = math.log2(math.e)
X_SWAP = [(0, 2), (2, 0), (1, 3), (3, 1)]
CORE_SWAP = [(0, 1), (1, 0), (2, 3), (3, 2)]
Y_SWAP = [(0, 1), (1, 0)]
Z_UP = [(0, 1), (1, 2), (2, 3), (3, 0)]
Z_DOWN = [(0, 3), (1, 0), (2, 1), (3, 2)]
Z_NEAR = [(0, 1), (1, 0), (2, 3), (3, 2)]
Z_FAR = [(0, 2), (2, 0), (1, 3), (3, 1)]
MASKS = (0, 2, 1, 3)
ANY = pl.BlockSpec(memory_space=pl.ANY)
SMEM = pl.BlockSpec(memory_space=pltpu.SMEM)


def fits(mesh):
    return dict(mesh.shape) == {"fsdp": 4, "ctx": 2, "tp": 4}


def dot(left, right, left_dim, right_dim):
    return lax.dot_general(
        left, right, (((left_dim,), (right_dim,)), ((), ())), preferred_element_type=F32
    )


def sigmoid(v):
    return 0.5 * jnp.tanh(0.5 * v) + 0.5


def whole(shape):
    zeros = (0,) * len(shape)
    return pl.BlockSpec(shape, lambda *_: zeros, pipeline_mode=pl.Buffered(1))


def settings(dims, mib):
    return pltpu.CompilerParams(
        dimension_semantics=("arbitrary",) * dims, vmem_limit_bytes=mib << 20
    )


def shape_of(shape, dtype):
    return jax.ShapeDtypeStruct(shape, dtype)


def cost(large, microseconds=None):
    size = 1 << 42 if large else 1 << 10
    if microseconds is not None:
        size = int(microseconds * 1.15e9)
    return pl.CostEstimate(flops=size, bytes_accessed=size >> 12, transcendentals=0)


def pack_kernel(info, o_in, g_in, u_in, d_in, *refs):
    out_ref, ffn_ref, *chunk_refs, others_ref, o_ref, g_ref, u_ref, d_ref, sems = refs
    ctx = info[2]
    pairs = ((o_in, o_ref), (g_in, g_ref), (u_in, u_ref), (d_in, d_ref))
    copies = [pltpu.make_async_copy(a, b, sems.at[i]) for i, (a, b) in enumerate(pairs)]
    for copy in copies:
        copy.start()
    for copy in copies:
        copy.wait()
    out_ref[...] = o_ref[...].astype(F32).T.astype(BF16)
    third = g_ref.shape[1] // 3
    for j in range(3):
        at = pl.multiple_of(jnp.where(ctx == 0, j, 2 - j) * third, third)
        parts = [
            g_ref[:, pl.ds(at, third)],
            u_ref[:, pl.ds(at, third)],
            d_ref[pl.ds(at, third), :].astype(F32).T.astype(BF16),
        ]
        for i, part in enumerate(parts):
            chunk_refs[j][:, i * third : (i + 1) * third] = part
            if j:
                others_ref[:, (3 * j - 3 + i) * third : (3 * j - 2 + i) * third] = part
            ffn_ref[:, (3 * j + i) * third : (3 * j + i + 1) * third] = part


def pack(info, o, g, u, d):
    rows, units = g.shape
    feats = o.shape[0]
    widths = (feats, 3 * units, units, units, units, 2 * units)
    return pl.pallas_call(
        pack_kernel,
        in_specs=[SMEM] + [ANY] * 4,
        out_specs=[pl.BlockSpec(memory_space=pltpu.VMEM)] * 6,
        out_shape=[shape_of((rows, n), BF16) for n in widths],
        scratch_shapes=[pltpu.VMEM(a.shape, BF16) for a in (o, g, u, d)]
        + [pltpu.SemaphoreType.DMA((4,))],
        compiler_params=pltpu.CompilerParams(vmem_limit_bytes=24 << 20),
        cost_estimate=cost(False),
        name="pack",
    )(info, o, g, u, d)


def join_kernel(q_ref, k_ref, v_ref, out_ref):
    at = 0
    for ref in (q_ref, k_ref, v_ref):
        out_ref[:, at : at + ref.shape[1]] = ref[...]
        at += ref.shape[1]


def join(q, k, v):
    return pl.pallas_call(
        join_kernel,
        out_shape=shape_of((q.shape[0], q.shape[1] + k.shape[1] + v.shape[1]), BF16),
        compiler_params=pltpu.CompilerParams(vmem_limit_bytes=8 << 20),
        cost_estimate=cost(False),
        name="join",
    )(q, k, v)


def norm_one_kernel(info, tok_ref, gain_ref, x_ref, nt_ref, x32):
    quarter = x_ref.shape[1] // 4
    for p, mask in enumerate(MASKS):
        at = pl.multiple_of(jnp.bitwise_xor(info[1], mask) * quarter, quarter)
        part = tok_ref[0, :, pl.ds(at, quarter)]
        x_ref[:, p * quarter : (p + 1) * quarter] = part
        x32[:, p * quarter : (p + 1) * quarter] = part.astype(F32)
    x = x32[...]
    rho = lax.rsqrt(jnp.mean(x * x, axis=-1, keepdims=True) + EPS)
    nt_ref[...] = (x * rho * gain_ref[...]).T.astype(BF16)


def norm_one(info, tokens, gain, tile):
    _, tok, width = tokens.shape
    return pl.pallas_call(
        norm_one_kernel,
        grid_spec=pltpu.PrefetchScalarGridSpec(
            num_scalar_prefetch=1,
            grid=(tok // tile,),
            in_specs=[
                pl.BlockSpec((1, tile, width), lambda i, info: (info[0], i, 0)),
                pl.BlockSpec((1, width), lambda i, info: (0, 0)),
            ],
            out_specs=[
                pl.BlockSpec((tile, width), lambda i, info: (i, 0)),
                pl.BlockSpec((width, tile), lambda i, info: (0, i)),
            ],
            scratch_shapes=[pltpu.VMEM((tile, width), F32)],
        ),
        out_shape=[shape_of((tok, width), BF16), shape_of((width, tok), BF16)],
        compiler_params=settings(1, 24),
        cost_estimate=cost(False),
        name="norm_one",
    )(info, tokens, gain)


def proj_kernel(heads, block, plan, count, info, *refs):
    nt_ref, cos_ref, sin_ref, qg_ref, kg_ref, rot_ref, raw_ref, w_ref, sem = refs[count:]
    rows = w_ref.shape[0] // 4

    @pl.when(pl.program_id(0) == 0)
    def _():
        for k in range(4):

            @pl.when(block(info) == k)
            def _():
                for p, (piece, row) in enumerate(plan[k]):
                    src = refs[piece].at[pl.ds(row, rows)]
                    pltpu.make_async_copy(src, w_ref.at[pl.ds(p * rows, rows)], sem).start()

        pltpu.make_async_copy(w_ref, w_ref, sem).wait()

    hd = qg_ref.shape[0]
    half = hd // 2
    raw = dot(w_ref[...], nt_ref[...], 0, 0)
    cos_part, sin_part = cos_ref[...], sin_ref[...]
    heads_q, heads_k = heads
    raw_ref[...] = raw.astype(BF16)
    for h in range(heads_q + heads_k):
        v = raw[h * hd : (h + 1) * hd]
        rho = lax.rsqrt(jnp.mean(v * v, axis=0, keepdims=True) + EPS)
        v = v * rho * (qg_ref[...] if h < heads_q else kg_ref[...])
        a, b = v[:half], v[half:]
        rot_ref[h * hd : h * hd + half, :] = (a * cos_part - b * sin_part).astype(BF16)
        rot_ref[h * hd + half : (h + 1) * hd, :] = (b * cos_part + a * sin_part).astype(BF16)
    at = (heads_q + heads_k) * hd
    rot_ref[at:, :] = raw[at:].astype(BF16)


def project(info, weights, normed_t, cos_part, sin_part, gain_q, gain_k, heads, block):
    plan, pieces = weights
    width, tok = normed_t.shape
    cols = pieces[0].shape[1]
    tile = min(512, tok)
    const = lambda a: pl.BlockSpec(a.shape, lambda i, info: (0, 0))
    tab = lambda a: pl.BlockSpec((a.shape[0], tile), lambda i, info: (0, i))
    return pl.pallas_call(
        functools.partial(proj_kernel, heads, block, plan, len(pieces)),
        grid_spec=pltpu.PrefetchScalarGridSpec(
            num_scalar_prefetch=1,
            grid=(tok // tile,),
            in_specs=[ANY] * len(pieces)
            + [tab(normed_t), tab(cos_part), tab(sin_part), const(gain_q), const(gain_k)],
            out_specs=[pl.BlockSpec((cols, tile), lambda i, info: (0, i))] * 2,
            scratch_shapes=[pltpu.VMEM((width, cols), BF16), pltpu.SemaphoreType.DMA],
        ),
        out_shape=[shape_of((cols, tok), BF16), shape_of((cols, tok), BF16)],
        compiler_params=settings(1, 24),
        cost_estimate=cost(False),
        name="project",
    )(info, *pieces, normed_t, cos_part, sin_part, gain_q, gain_k)


def head_back_kernel(
    heads, info, dm_ref, dt_ref, rm_ref, rt_ref, cos_ref, sin_ref, qg_ref, kg_ref, out_ref, gg_ref
):
    step, part = pl.program_id(0), pl.program_id(1)
    hd = qg_ref.shape[0]
    half = hd // 2
    heads_q, heads_k = heads
    cos_part, sin_part = cos_ref[...], sin_ref[...]
    tile = cos_part.shape[1]

    @pl.when((step == 0) & (part == 0))
    def _():
        gg_ref[...] = jnp.zeros_like(gg_ref)

    def work(d_ref, r_ref):
        gain_q = jnp.zeros((hd, 1), F32)
        gain_k = jnp.zeros((hd, 1), F32)
        done = []
        for h in range(heads_q + heads_k):
            is_q = h < heads_q
            g = d_ref[h * hd : (h + 1) * hd, :].astype(F32)
            raw = r_ref[h * hd : (h + 1) * hd, :].astype(F32)
            a, b = g[:half], g[half:]
            turned = jnp.concatenate(
                [a * cos_part + b * sin_part, b * cos_part - a * sin_part], axis=0
            )
            rho = lax.rsqrt(jnp.mean(raw * raw, axis=0, keepdims=True) + EPS)
            unit = raw * rho
            prod = turned * unit
            scaled = turned * (qg_ref[...] if is_q else kg_ref[...])
            mean = jnp.mean(scaled * unit, axis=0, keepdims=True)
            done.append(rho * (scaled - unit * mean))
            total = jnp.sum(prod, axis=1, keepdims=True)
            if is_q:
                gain_q = gain_q + total
            else:
                gain_k = gain_k + total
        done.append(d_ref[(heads_q + heads_k) * hd :, :].astype(F32))
        out_ref[0] = jnp.concatenate(done, axis=0).T.astype(BF16)
        lane = lax.broadcasted_iota(jnp.int32, gg_ref.shape, 1)
        gg_ref[...] += jnp.where(lane == 0, gain_q, jnp.where(lane == 1, gain_k, 0.0))

    @pl.when(step == 0)
    def _():
        work(dm_ref, rm_ref)

    @pl.when(step == 1)
    def _():
        work(dt_ref, rt_ref)


def head_back(info, grad_mine, grad_theirs, raw_mine, raw_theirs, cos_part, sin_part, gq, gk, heads):
    cols, tok = grad_mine.shape
    tile = min(512, tok)
    mine = pl.BlockSpec((cols, tile), lambda s, i, info: (0, jnp.where(s == 0, i, tok // tile - 1)))
    theirs = pl.BlockSpec((cols, tile), lambda s, i, info: (0, jnp.where(s == 0, 0, i)))
    tab = lambda a: pl.BlockSpec((a.shape[0], tile), lambda s, i, info: (0, i))
    const = lambda a: pl.BlockSpec(a.shape, lambda s, i, info: (0, 0))
    return pl.pallas_call(
        functools.partial(head_back_kernel, heads),
        grid_spec=pltpu.PrefetchScalarGridSpec(
            num_scalar_prefetch=1,
            grid=(2, tok // tile),
            in_specs=[
                mine,
                theirs,
                mine,
                theirs,
                tab(cos_part),
                tab(sin_part),
                const(gq),
                const(gk),
            ],
            out_specs=[
                pl.BlockSpec(
                    (1, tile, cols), lambda s, i, info: (jnp.bitwise_xor(info[2], s), i, 0)
                ),
                pl.BlockSpec((gq.shape[0], 128), lambda s, i, info: (0, 0)),
            ],
        ),
        out_shape=[shape_of((2, tok, cols), BF16), shape_of((gq.shape[0], 128), F32)],
        compiler_params=settings(2, 60),
        cost_estimate=cost(False),
        name="head_back",
    )(info, grad_mine, grad_theirs, raw_mine, raw_theirs, cos_part, sin_part, gq, gk)


def load_rows(info, mine_ref, got_ref, rows, sems):
    tok = mine_ref.shape[1]
    ctx = info[2]
    here = pl.multiple_of(ctx * tok, tok)
    there = pl.multiple_of((1 - ctx) * tok, tok)
    one = pltpu.make_async_copy(mine_ref, rows.at[:, pl.ds(here, tok)], sems.at[0])
    two = pltpu.make_async_copy(got_ref, rows.at[:, pl.ds(there, tok)], sems.at[1])
    one.start()
    two.start()
    one.wait()
    two.wait()


def keys_with_bias(keys, length):
    hd, slots = keys.shape
    pos = lax.broadcasted_iota(jnp.int32, (hd, slots), 1)
    row = lax.broadcasted_iota(jnp.int32, (hd, slots), 0)
    bias = jnp.where((row == 0) & (pos >= length), NEGATIVE, 0.0)
    return jnp.concatenate([keys.astype(F32), bias], axis=0).T.astype(BF16)


def query_with_one(pair):
    one_row = jnp.where(lax.broadcasted_iota(jnp.int32, pair.shape, 0) == 0, 1.0, 0.0)
    return jnp.concatenate([pair, one_row.astype(BF16)], axis=0)


def by_halves(left, right):
    half = left.shape[1] // 2
    return jnp.concatenate(
        [left[:, :half], right[:, :half], left[:, half:], right[:, half:]], axis=1
    )


def by_heads(both):
    quarter = both.shape[1] // 4
    part = lambda i: both[:, i * quarter : (i + 1) * quarter]
    return (
        jnp.concatenate([part(0), part(2)], axis=1),
        jnp.concatenate([part(1), part(3)], axis=1),
    )


def causal(scores):
    half = scores.shape[0]
    key_pos = lax.broadcasted_iota(jnp.int32, (half, half), 0)
    query_pos = lax.broadcasted_iota(jnp.int32, (half, half), 1)
    allowed = key_pos <= query_pos
    return jnp.where(jnp.concatenate([allowed, allowed], axis=1), scores, NEGATIVE)


def attn_fwd_kernel(
    width, hd, info, mine_ref, got_ref, keep_ref, send_ref, lse_ref, rows, key_rows, sems
):
    head, block = pl.program_id(0), pl.program_id(1)
    heads_k = pl.num_programs(0)
    scale = hd**-0.5 * LOG2E
    length = info[3]
    key_at = pl.multiple_of(heads_k * 2 * hd + head * hd, hd)
    value_at = pl.multiple_of(heads_k * 3 * hd + head * hd, hd)
    query_at = pl.multiple_of(head * 2 * hd, 2 * hd)

    @pl.when((head == 0) & (block == 0))
    def _():
        load_rows(info, mine_ref, got_ref, rows, sems)

    @pl.when(block == 0)
    def _():
        key_rows[...] = keys_with_bias(rows[pl.ds(key_at, hd), :], length)

    start = pl.multiple_of(block * width, width)
    both = rows[pl.ds(query_at, 2 * hd), pl.ds(start, width)]
    query = query_with_one(by_halves(both[:hd], both[hd:]))

    def tile(at, carried, diagonal):
        out, total = carried
        scores = dot(key_rows[pl.ds(at, width), :], query, 1, 0)
        if diagonal:
            key_pos = lax.broadcasted_iota(jnp.int32, (width, width), 0)
            query_pos = lax.broadcasted_iota(jnp.int32, (width, width), 1)
            allowed = key_pos <= query_pos
            allowed = by_halves(allowed, allowed)
            scores = jnp.where(allowed, scores, NEGATIVE)
        probs = jnp.exp2(scores * scale)
        total = total + jnp.sum(probs, axis=0, keepdims=True)
        out = out + dot(rows[pl.ds(value_at, hd), pl.ds(at, width)], probs.astype(BF16), 1, 0)
        return out, total

    carried = (jnp.zeros((hd, 2 * width), F32), jnp.zeros((1, 2 * width), F32))
    full = jnp.minimum(block, lax.div(length + width - 1, width))
    carried = lax.fori_loop(
        0, full, lambda j, c: tile(pl.multiple_of(j * width, width), c, False), carried
    )
    out, total = tile(start, carried, True)
    out = out * (1.0 / total)
    out = jnp.concatenate(by_heads(out), axis=0).T.astype(BF16)
    here = block // 2 == info[2]

    @pl.when(here)
    def _():
        keep_ref[...] = out

    @pl.when(jnp.logical_not(here))
    def _():
        send_ref[...] = out

    log_first, log_second = by_heads(jnp.log2(total))
    lse_ref[0, 0:1, :] = log_first
    lse_ref[0, 1:2, :] = log_second


def keep_block(i, info):
    return jnp.clip(i - 2 * info[2], 0, 1)


def send_block(i, info):
    return jnp.clip(i - 2 * (1 - info[2]), 0, 1)


def attn_fwd(info, mine, got, hd):
    cols, tok = mine.shape
    heads_k = cols // (4 * hd)
    width = tok // 2
    return pl.pallas_call(
        functools.partial(attn_fwd_kernel, width, hd),
        grid_spec=pltpu.PrefetchScalarGridSpec(
            num_scalar_prefetch=1,
            grid=(heads_k, 4),
            in_specs=[ANY, ANY],
            out_specs=[
                pl.BlockSpec((width, 2 * hd), lambda h, i, info: (keep_block(i, info), h)),
                pl.BlockSpec((width, 2 * hd), lambda h, i, info: (send_block(i, info), h)),
                pl.BlockSpec((1, 2, width), lambda h, i, info: (h, 0, i)),
            ],
            scratch_shapes=[
                pltpu.VMEM((cols, 2 * tok), BF16),
                pltpu.VMEM((2 * tok, 2 * hd), BF16),
                pltpu.SemaphoreType.DMA((2,)),
            ],
        ),
        out_shape=[
            shape_of((tok, heads_k * 2 * hd), BF16),
            shape_of((tok, heads_k * 2 * hd), BF16),
            shape_of((heads_k, 2, 2 * tok), F32),
        ],
        compiler_params=settings(2, 60),
        cost_estimate=cost(True),
        name="attn_fwd",
    )(info, mine, got)


def attn_bwd_kernel(
    width,
    hd,
    info,
    mine_ref,
    got_ref,
    ok_ref,
    os_ref,
    gk_ref,
    gs_ref,
    lse_ref,
    keep_ref,
    send_ref,
    rows,
    key_rows,
    value_rows,
    key_sum,
    value_sum,
    sems,
):
    head, block = pl.program_id(0), pl.program_id(1)
    heads_k = pl.num_programs(0)
    scale = hd**-0.5
    length = info[3]
    ctx = info[2]
    tok = keep_ref.shape[1]
    key_at = pl.multiple_of(heads_k * 2 * hd + head * hd, hd)
    value_at = pl.multiple_of(heads_k * 3 * hd + head * hd, hd)
    query_at = pl.multiple_of(head * 2 * hd, 2 * hd)

    @pl.when((head == 0) & (block == 0))
    def _():
        load_rows(info, mine_ref, got_ref, rows, sems)

    @pl.when(block == 0)
    def _():
        key_rows[...] = keys_with_bias(rows[pl.ds(key_at, hd), :], length)
        value_rows[...] = rows[pl.ds(value_at, hd), :].astype(F32).T.astype(BF16)
        key_sum[...] = jnp.zeros_like(key_sum)
        value_sum[...] = jnp.zeros_like(value_sum)

    start = pl.multiple_of(block * width, width)
    here = block // 2 == ctx

    def store_query(value):
        at = pl.ds(pl.multiple_of((block % 2) * width, width), width)

        @pl.when(here)
        def _():
            keep_ref[pl.ds(query_at, 2 * hd), at] = value

        @pl.when(jnp.logical_not(here))
        def _():
            send_ref[pl.ds(query_at, 2 * hd), at] = value

    @pl.when(block * width < length)
    def _():
        both = rows[pl.ds(query_at, 2 * hd), pl.ds(start, width)]
        pair = by_halves(both[:hd], both[hd:])
        query = query_with_one(pair)
        query_rows = pair.astype(F32).T.astype(BF16)
        grad_wide = jnp.where(here, gk_ref[...].astype(F32), gs_ref[...].astype(F32))
        out_wide = jnp.where(here, ok_ref[...].astype(F32), os_ref[...].astype(F32))
        grad_t = grad_wide.T
        prod = (grad_wide * out_wide).T
        grad = by_halves(grad_t[:hd], grad_t[hd:]).astype(BF16)
        half = width // 2
        grad_rows = jnp.concatenate(
            [
                grad_wide[:half, :hd],
                grad_wide[:half, hd:],
                grad_wide[half:, :hd],
                grad_wide[half:, hd:],
            ],
            axis=0,
        ).astype(BF16)
        delta = by_halves(
            jnp.sum(prod[:hd], axis=0, keepdims=True), jnp.sum(prod[hd:], axis=0, keepdims=True)
        )
        lse = by_halves(lse_ref[0, 0:1, :], lse_ref[0, 1:2, :])

        def terms(at, keys, first, mask):
            scores = dot(key_rows[pl.ds(at, keys), :], query[:, first:], 1, 0)
            if mask:
                part = causal(scores[:, :width])
                wide = scores.shape[1] > width
                scores = jnp.concatenate([part, scores[:, width:]], axis=1) if wide else part
            probs = jnp.exp2(scores * (scale * LOG2E) - lse[:, first:])
            grad_probs = dot(value_rows[pl.ds(at, keys), :], grad[:, first:], 1, 0)
            grad_scores = (probs * (grad_probs - delta[:, first:])).astype(BF16)
            value_sum[pl.ds(at, keys), :] += dot(probs.astype(BF16), grad_rows[first:], 1, 0)
            key_sum[pl.ds(at, keys), :] += dot(grad_scores, query_rows[first:], 1, 0)
            return dot(rows[pl.ds(key_at, hd), pl.ds(at, keys)], grad_scores, 1, 0)

        query_sum = lax.fori_loop(
            0,
            block,
            lambda j, s: s + terms(pl.multiple_of(j * width, width), width, 0, False),
            jnp.zeros((hd, 2 * width), F32),
        )
        query_sum = query_sum + terms(start, half, 0, True)
        later = terms(pl.multiple_of(start + half, half), half, width, True)
        query_sum = jnp.concatenate([query_sum[:, :width], query_sum[:, width:] + later], axis=1)
        store_query(jnp.concatenate(by_heads(query_sum * scale), axis=0).astype(BF16))

    @pl.when(block * width >= length)
    def _():
        store_query(jnp.zeros((2 * hd, width), BF16))

    @pl.when(block == 3)
    def _():
        for at, total in ((key_at, key_sum[...] * scale), (value_at, value_sum[...])):
            total = total.T.astype(BF16)
            left, right = total[:, :tok], total[:, tok:]

            @pl.when(ctx == 0)
            def _():
                keep_ref[pl.ds(at, hd), :] = left
                send_ref[pl.ds(at, hd), :] = right

            @pl.when(ctx == 1)
            def _():
                keep_ref[pl.ds(at, hd), :] = right
                send_ref[pl.ds(at, hd), :] = left


def attn_bwd(info, mine, got, out_keep, out_send, grad_keep, grad_send, lse, hd):
    cols, tok = mine.shape
    heads_k = cols // (4 * hd)
    width = tok // 2
    keep = pl.BlockSpec((width, 2 * hd), lambda h, i, info: (keep_block(i, info), h))
    send = pl.BlockSpec((width, 2 * hd), lambda h, i, info: (send_block(i, info), h))
    full = pl.BlockSpec((cols, tok), lambda h, i, info: (0, 0))
    return pl.pallas_call(
        functools.partial(attn_bwd_kernel, width, hd),
        grid_spec=pltpu.PrefetchScalarGridSpec(
            num_scalar_prefetch=1,
            grid=(heads_k, 4),
            in_specs=[
                ANY,
                ANY,
                keep,
                send,
                keep,
                send,
                pl.BlockSpec((1, 2, width), lambda h, i, info: (h, 0, i)),
            ],
            out_specs=[full, full],
            scratch_shapes=[
                pltpu.VMEM((cols, 2 * tok), BF16),
                pltpu.VMEM((2 * tok, 2 * hd), BF16),
                pltpu.VMEM((2 * tok, hd), BF16),
                pltpu.VMEM((2 * tok, hd), F32),
                pltpu.VMEM((2 * tok, hd), F32),
                pltpu.SemaphoreType.DMA((2,)),
            ],
        ),
        out_shape=[shape_of((cols, tok), BF16), shape_of((cols, tok), BF16)],
        compiler_params=settings(2, 60),
        cost_estimate=cost(True, 16.2),
        name="attn_bwd",
    )(info, mine, got, out_keep, out_send, grad_keep, grad_send, lse)


def load_blocks(plan, pieces, target, sem):
    rows = target.shape[1] // 4

    @pl.when(pl.program_id(0) == 0)
    def _():
        for k, places in enumerate(plan):
            for p, (piece, row) in enumerate(places):
                src = pieces[piece].at[pl.ds(row, rows)]
                pltpu.make_async_copy(src, target.at[k, pl.ds(p * rows, rows)], sem).start()
        pltpu.make_async_copy(target, target, sem).wait()


def out_proj_kernel(plan, count, info, *refs):
    x_ref, a0, a1, b0, b1, gain_ref, r_ref, n_ref, nt_ref, att_ref, w_ref, sem = refs[count:]
    load_blocks(plan, refs, w_ref, sem)
    ctx = info[2]
    total = x_ref[...].astype(F32)
    for j, ref, side in ((0, a0, ctx), (1, a1, ctx), (0, b0, 1 - ctx), (1, b1, 1 - ctx)):
        block = 2 * side + j
        part = ref[...]
        att_ref[block] = part
        total = total + dot(part, w_ref[block], 1, 1)
    rho = lax.rsqrt(jnp.mean(total * total, axis=-1, keepdims=True) + EPS)
    normed = total * rho * gain_ref[...]
    r_ref[...] = total
    n_ref[...] = normed.astype(BF16)
    nt_ref[...] = normed.T.astype(BF16)


def out_proj(info, x, mine, theirs, weights, gain, tile):
    plan, pieces = weights
    tok, width = x.shape
    feats = pieces[0].shape[1]
    rows_of = lambda n: pl.BlockSpec((tile, n), lambda i, info: (i, 0))
    return pl.pallas_call(
        functools.partial(out_proj_kernel, plan, len(pieces)),
        grid_spec=pltpu.PrefetchScalarGridSpec(
            num_scalar_prefetch=1,
            grid=(tok // tile,),
            in_specs=[ANY] * len(pieces)
            + [rows_of(width)]
            + [rows_of(feats)] * 4
            + [pl.BlockSpec((1, width), lambda i, info: (0, 0))],
            out_specs=[
                rows_of(width),
                rows_of(width),
                pl.BlockSpec((width, tile), lambda i, info: (0, i)),
                pl.BlockSpec((4, tile, feats), lambda i, info: (0, i, 0)),
            ],
            scratch_shapes=[pltpu.VMEM((4, width, feats), BF16), pltpu.SemaphoreType.DMA],
        ),
        out_shape=[
            shape_of((tok, width), F32),
            shape_of((tok, width), BF16),
            shape_of((width, tok), BF16),
            shape_of((4, tok, feats), BF16),
        ],
        compiler_params=settings(1, 60),
        cost_estimate=cost(True),
        name="out_proj",
    )(info, *pieces, x, *mine, *theirs, gain)


def norm_two_back_kernel(plan, count, info, *refs):
    g_ref, r_ref, gr_ref, gain_ref, gres_ref, gat_ref, a0, a1, b0, b1, gg_ref, w_ref, sem = refs[count:]
    load_blocks(plan, refs, w_ref, sem)
    ctx = info[2]
    grad, resid = g_ref[...], r_ref[...]
    rho = lax.rsqrt(jnp.mean(resid * resid, axis=-1, keepdims=True) + EPS)
    unit = resid * rho
    scaled = grad * gain_ref[...]
    back = rho * (scaled - unit * jnp.mean(scaled * unit, axis=-1, keepdims=True))
    total = gr_ref[...] + back
    gres_ref[...] = total
    low = total.astype(BF16)
    gat_ref[...] = total.T.astype(BF16)

    @pl.when(pl.program_id(0) == 0)
    def _():
        gg_ref[...] = jnp.zeros_like(gg_ref)

    gg_ref[...] += jnp.sum(grad * unit, axis=0, keepdims=True)
    for j, ref, side in ((0, a0, ctx), (1, a1, ctx), (0, b0, 1 - ctx), (1, b1, 1 - ctx)):
        ref[...] = dot(low, w_ref[2 * side + j], 1, 0).astype(BF16)


def norm_two_back(info, grad, resid, grad_result, gain, weights, tile):
    plan, pieces = weights
    tok, width = grad.shape
    feats = pieces[0].shape[1]
    rows_of = lambda n: pl.BlockSpec((tile, n), lambda i, info: (i, 0))
    row = pl.BlockSpec((1, width), lambda i, info: (0, 0))
    return pl.pallas_call(
        functools.partial(norm_two_back_kernel, plan, len(pieces)),
        grid_spec=pltpu.PrefetchScalarGridSpec(
            num_scalar_prefetch=1,
            grid=(tok // tile,),
            in_specs=[ANY] * len(pieces) + [rows_of(width)] * 3 + [row],
            out_specs=[rows_of(width), pl.BlockSpec((width, tile), lambda i, info: (0, i))]
            + [rows_of(feats)] * 4
            + [row],
            scratch_shapes=[pltpu.VMEM((4, width, feats), BF16), pltpu.SemaphoreType.DMA],
        ),
        out_shape=[shape_of((tok, width), F32), shape_of((width, tok), BF16)]
        + [shape_of((tok, feats), BF16)] * 4
        + [shape_of((1, width), F32)],
        compiler_params=settings(1, 60),
        cost_estimate=cost(True, 5.4),
        name="norm_two_back",
    )(info, *pieces, grad, resid, grad_result, gain)


def norm_one_back_kernel(plan, count, info, *refs):
    p0, p1, x_ref, gres_ref, gain_ref, out_ref, gg_ref, w_ref, sem = refs[count:]
    load_blocks(plan, refs, w_ref, sem)
    quarter = x_ref.shape[1] // 4
    grad = dot(p0[0], w_ref[0], 1, 1)
    grad = grad + dot(p1[0], w_ref[1], 1, 1)
    grad = grad + dot(p0[1], w_ref[2], 1, 1)
    grad = grad + dot(p1[1], w_ref[3], 1, 1)
    x = x_ref[...].astype(F32)
    rho = lax.rsqrt(jnp.mean(x * x, axis=-1, keepdims=True) + EPS)
    unit = x * rho
    scaled = grad * gain_ref[...]
    back = rho * (scaled - unit * jnp.mean(scaled * unit, axis=-1, keepdims=True))
    total = (gres_ref[...] + back).astype(BF16)
    for p, mask in enumerate(MASKS):
        at = pl.multiple_of(jnp.bitwise_xor(info[1], mask) * quarter, quarter)
        part = total[:, p * quarter : (p + 1) * quarter]

        out_ref[:, pl.ds(at, quarter)] = part

    @pl.when(pl.program_id(0) == 0)
    def _():
        gg_ref[...] = jnp.zeros_like(gg_ref)

    gg_ref[...] += jnp.sum(grad * unit, axis=0, keepdims=True)


def norm_one_back(info, pairs, weights, x, grad_resid, gain, tile, part):
    plan, pieces = weights
    tok, width = x.shape
    cols = pieces[0].shape[1]
    steps = tok // tile // 2
    first = part * steps
    rows_of = lambda n: pl.BlockSpec((tile, n), lambda i, info: (first + i, 0))
    out_rows = pl.BlockSpec((tile, width), lambda i, info: (i, 0))
    pair = pl.BlockSpec((2, tile, cols), lambda i, info: (0, first + i, 0))
    row = pl.BlockSpec((1, width), lambda i, info: (0, 0))
    return pl.pallas_call(
        functools.partial(norm_one_back_kernel, plan, len(pieces)),
        grid_spec=pltpu.PrefetchScalarGridSpec(
            num_scalar_prefetch=1,
            grid=(steps,),
            in_specs=[ANY] * len(pieces) + [pair, pair, rows_of(width), rows_of(width), row],
            out_specs=[out_rows, row],
            scratch_shapes=[pltpu.VMEM((4, width, cols), BF16), pltpu.SemaphoreType.DMA],
        ),
        out_shape=[shape_of((tok // 2, width), BF16), shape_of((1, width), F32)],
        compiler_params=settings(1, 60),
        cost_estimate=cost(True),
        name="norm_one_back",
    )(info, *pieces, *pairs, x, grad_resid, gain)


def weight_copies(plan, pieces, gate_up, down, gate_up_sem, down_sem):
    third = down.shape[1] // 3
    rows = down.shape[0] // 4
    wide, thin = [], []
    for p, chunks in enumerate(plan):
        block = pl.ds(p * rows, rows)
        for j, (piece, row, at) in enumerate(chunks):
            src = pieces[piece].at[pl.ds(row, rows)]
            wide.append(
                pltpu.make_async_copy(
                    src.at[:, pl.ds(at, 2 * third)],
                    gate_up.at[block, pl.ds(j * 2 * third, 2 * third)],
                    gate_up_sem,
                )
            )
            thin.append(
                pltpu.make_async_copy(
                    src.at[:, pl.ds(at + 2 * third, third)],
                    down.at[block, pl.ds(j * third, third)],
                    down_sem,
                )
            )
    return wide, thin


def split_act(act):
    third = act.shape[1] // 6
    part = lambda j: act[:, j * third : (j + 1) * third]
    return [(part(0), part(1)), (part(2), part(3)), (part(4), part(5))]


def ffn_fwd_kernel(tile, plans, last, info, scale, x_ref, in_ref, *rest):
    if last:
        teach_ref, rest = rest[0], rest[1:]
    pieces = []
    for plan in plans:
        count = 1 + max(place[0] for chunks in plan for place in chunks)
        pieces.append(rest[:count])
        rest = rest[count:]
    act_ref, hid_ref = rest[:2]
    if last:
        out_ref, gres_ref, low_ref, lowt_ref, sq_ref = rest[2:7]
        gate_up, down, total, sems = rest[7:]
    else:
        sum_ref, gate_up, down, total, sems = rest[2:]
    step, part = pl.program_id(0), pl.program_id(1)
    final = len(plans) - 1
    width = x_ref.shape[1]
    quarter = width // 4
    third = down.shape[2] // 3

    def copies(s):
        return weight_copies(
            plans[s], pieces[s], gate_up.at[s], down.at[s], sems.at[s, 0], sems.at[s, 1]
        )

    @pl.when((step == 0) & (part == 0))
    def _():
        for s in range(len(plans)):
            wide, thin = copies(s)
            for copy in wide + thin:
                copy.start()

    for s in range(len(plans)):

        @pl.when((step == s) & (part == 0))
        def _():
            pltpu.make_async_copy(gate_up.at[s], gate_up.at[s], sems.at[s, 0]).wait()

    rows = pl.ds(pl.multiple_of(part * tile, tile), tile)
    act = dot(x_ref[rows, :], gate_up[step], 1, 0)
    for j, (gate, upper) in enumerate(split_act(act)):
        sig = sigmoid(gate)
        silu = gate * sig
        hid_ref[0, :, j * third : (j + 1) * third] = (silu * upper).astype(BF16)
        at = 2 * j * third
        act_ref[0, :, at : at + third] = (upper * (sig + silu - silu * sig)).astype(BF16)
        act_ref[0, :, at + third : at + 2 * third] = silu.astype(BF16)
    for s in range(len(plans)):

        @pl.when((step == s) & (part == 0))
        def _():
            pltpu.make_async_copy(down.at[s], down.at[s], sems.at[s, 1]).wait()

    grown = dot(hid_ref[0], down[step], 1, 1)

    @pl.when(step == 0)
    def _():
        total[rows, :] = in_ref[...] + grown

    @pl.when(step > 0)
    def _():
        total[rows, :] += grown

    @pl.when(step == final)
    def _():
        result = total[rows, :]
        if not last:
            sum_ref[...] = result
            return
        tok = x_ref.shape[0]
        slot = info[2] * tok + part * tile + lax.broadcasted_iota(jnp.int32, (tile, 1), 0)
        valid = jnp.where(slot < info[3], 1.0, 0.0)
        square = jnp.zeros((tile, quarter), F32)
        for p, mask in enumerate(MASKS):
            at = pl.multiple_of(jnp.bitwise_xor(info[1], mask) * quarter, quarter)
            cols = slice(p * quarter, (p + 1) * quarter)
            value = result[:, cols]
            out_ref[:, pl.ds(at, quarter)] = value.astype(BF16)
            error = valid * (value - teach_ref[0, :, pl.ds(at, quarter)].astype(F32))
            square = square + error * error
            grad = error * scale[0]
            gres_ref[:, cols] = grad
            low_ref[:, cols] = grad.astype(BF16)
            lowt_ref[cols, :] = grad.T.astype(BF16)

        @pl.when(part == 0)
        def _():
            sq_ref[...] = jnp.zeros_like(sq_ref)

        sq_ref[...] += jnp.sum(square, axis=0, keepdims=True)


def ffn_fwd(info, scale, x, total, teacher, weights, units, tile):
    tok, width = x.shape
    pieces = [piece for _, group in weights for piece in group]
    count = len(weights)
    last = teacher is not None
    entry = lambda s, i: jnp.where(s == 0, i, tok // tile - 1)
    leave = lambda s, i: jnp.where(s == count - 1, i, 0)
    tiles = lambda n: pl.BlockSpec((tile, n), lambda s, i, info: (leave(s, i), 0))
    slab = lambda n: pl.BlockSpec((1, tile, n), lambda s, i, info: (s, i, 0))
    in_specs = [
        SMEM,
        whole((tok, width)),
        pl.BlockSpec((tile, width), lambda s, i, info: (entry(s, i), 0)),
    ]
    out_specs = [slab(2 * units), slab(units)]
    out_shape = [shape_of((count, tok, 2 * units), BF16), shape_of((count, tok, units), BF16)]
    if last:
        in_specs.append(
            pl.BlockSpec((1, tile, width), lambda s, i, info: (info[0], leave(s, i), 0))
        )
        out_specs += [
            tiles(width),
            tiles(width),
            tiles(width),
            pl.BlockSpec((width, tile), lambda s, i, info: (0, leave(s, i))),
            pl.BlockSpec((1, width // 4), lambda s, i, info: (0, 0)),
        ]
        out_shape += [
            shape_of((tok, width), BF16),
            shape_of((tok, width), F32),
            shape_of((tok, width), BF16),
            shape_of((width, tok), BF16),
            shape_of((1, width // 4), F32),
        ]
    else:
        out_specs.append(tiles(width))
        out_shape.append(shape_of((tok, width), F32))
    return pl.pallas_call(
        functools.partial(ffn_fwd_kernel, tile, [plan for plan, _ in weights], last),
        grid_spec=pltpu.PrefetchScalarGridSpec(
            num_scalar_prefetch=1,
            grid=(count, tok // tile),
            in_specs=in_specs + [ANY] * len(pieces),
            out_specs=out_specs,
            scratch_shapes=[
                pltpu.VMEM((count, width, 2 * units), BF16),
                pltpu.VMEM((count, width, units), BF16),
                pltpu.VMEM((tok, width), F32),
                pltpu.SemaphoreType.DMA((count, 2)),
            ],
        ),
        out_shape=out_shape,
        compiler_params=settings(2, 60),
        cost_estimate=cost(True),
        name="ffn_fwd",
    )(info, scale, x, total, *([teacher] if last else []), *pieces)


def ffn_bwd_kernel(steps, plan, first, low_ref, act_ref, hid_ref, xt_ref, lowt_ref, *rest):
    count = 1 + max(place[0] for chunks in plan for place in chunks)
    pieces, rest = rest[:count], rest[count:]
    if not first:
        in_ref, rest = rest[0], rest[1:]
    out_ref, keep_ref, send_ref, gate_up, down, dact_all, hid_all, sems = rest
    step = pl.program_id(0)
    units = down.shape[1]
    third = units // 3
    tile = low_ref.shape[0]

    @pl.when(step == 0)
    def _():
        wide, thin = weight_copies(plan, pieces, gate_up, down, sems.at[0], sems.at[1])
        for copy in thin + wide:
            copy.start()
        pltpu.make_async_copy(down, down, sems.at[1]).wait()

    @pl.when(step < steps)
    def _():
        rows = pl.ds(pl.multiple_of(step * tile, tile), tile)
        grad_hidden = dot(low_ref[...], down[...], 1, 0)
        for j, (to_gate, to_upper) in enumerate(split_act(act_ref[0])):
            grad = grad_hidden[:, j * third : (j + 1) * third]
            at = 2 * j * third
            dact_all[rows, at : at + third] = (grad * to_gate.astype(F32)).astype(BF16)
            dact_all[rows, at + third : at + 2 * third] = (grad * to_upper.astype(F32)).astype(BF16)
        hid_all[rows, :] = hid_ref[0]

        @pl.when(step == 0)
        def _():
            pltpu.make_async_copy(gate_up, gate_up, sems.at[0]).wait()

        grown = dot(dact_all[rows, :], gate_up[...], 1, 1)
        out_ref[...] = grown if first else in_ref[...] + grown

    def weight_rows(target):
        target[:, : 2 * units] = dot(xt_ref[...], dact_all[...], 1, 0).astype(BF16)
        target[:, 2 * units :] = dot(lowt_ref[...], hid_all[...], 1, 0).astype(BF16)

    @pl.when((step >= steps) & (step < steps + 2))
    def _():
        weight_rows(send_ref)

    @pl.when(step >= steps + 2)
    def _():
        weight_rows(keep_ref)


def ffn_bwd(low, saved, weights, total, xt, lowt, tile):
    plan, pieces = weights
    acts, hiddens, block = saved
    tok, width = low.shape
    units = hiddens.shape[2]
    steps = tok // tile
    quarter = width // 4
    first = total is None
    clip = lambda i: jnp.minimum(i, steps - 1)
    rows_of = lambda n: pl.BlockSpec((tile, n), lambda i: (clip(i), 0))
    slab = lambda n: pl.BlockSpec((1, tile, n), lambda i: (block, clip(i), 0))
    feature = lambda i: (jnp.where(i < steps + 2, jnp.maximum(i - steps, 0) + 2, i - steps - 2), 0)
    return pl.pallas_call(
        functools.partial(ffn_bwd_kernel, steps, plan, first),
        grid=(steps + 4,),
        in_specs=[
            rows_of(width),
            slab(2 * units),
            slab(units),
            pl.BlockSpec((quarter, tok), feature),
            pl.BlockSpec((quarter, tok), feature),
        ]
        + [ANY] * len(pieces)
        + ([] if first else [rows_of(width)]),
        out_specs=[
            rows_of(width),
            pl.BlockSpec((quarter, 3 * units), lambda i: (jnp.maximum(i - steps - 2, 0), 0)),
            pl.BlockSpec((quarter, 3 * units), lambda i: (jnp.clip(i - steps, 0, 1), 0)),
        ],
        out_shape=[
            shape_of((tok, width), F32),
            shape_of((width // 2, 3 * units), BF16),
            shape_of((width // 2, 3 * units), BF16),
        ],
        scratch_shapes=[
            pltpu.VMEM((width, 2 * units), BF16),
            pltpu.VMEM((width, units), BF16),
            pltpu.VMEM((tok, 2 * units), BF16),
            pltpu.VMEM((tok, units), BF16),
            pltpu.SemaphoreType.DMA((2,)),
        ],
        input_output_aliases={} if first else {5 + len(pieces): 0},
        compiler_params=settings(1, 60),
        cost_estimate=cost(True, 11.2),
        name="ffn_bwd",
    )(low, acts, hiddens, xt, lowt, *pieces, *([] if first else [total]))


def turn_chunks(block):
    wide = block.shape[1] * 2 // 9
    thin = wide // 2
    starts = [(2 * wide, wide), (wide, wide), (0, wide)]
    starts += [(3 * wide + 2 * thin, thin), (3 * wide + thin, thin), (3 * wide, thin)]
    return jnp.concatenate([block[:, a : a + n] for a, n in starts], axis=1)


def sum_kernel(turns, *refs):
    total = None
    for ref, turn in zip(refs[:-1], turns):
        value = ref[...].astype(F32)
        value = turn_chunks(value) if turn else value
        total = value if total is None else total + value
    refs[-1][...] = total.astype(refs[-1].dtype)


def summed(terms, turns=None, dtype=BF16):
    rows, cols = terms[0].shape
    spec = pl.BlockSpec((128, cols), lambda i: (i, 0))
    return pl.pallas_call(
        functools.partial(sum_kernel, turns or [False] * len(terms)),
        grid=(rows // 128,),
        in_specs=[spec] * len(terms),
        out_specs=spec,
        out_shape=shape_of((rows, cols), dtype),
        compiler_params=settings(1, 60),
        cost_estimate=cost(False),
        name="summed",
    )(*terms)


def sums_kernel(jobs, count, info, *refs):
    arrays, refs = refs[:count], refs[count:]
    outs, (term_buf, out_buf, term_sems, out_sems) = refs[: len(jobs)], refs[len(jobs) :]
    rows = term_buf.shape[1]
    copies = []
    for terms in jobs:
        group = []
        for array, base, pick, _ in terms:
            at = base
            if pick is not None:
                at = pl.multiple_of(base + jnp.bitwise_xor(info[2], pick) * rows, rows)
            i = len(copies) + len(group)
            src = arrays[array].at[pl.ds(at, rows)]
            group.append(pltpu.make_async_copy(src, term_buf.at[i], term_sems.at[i]))
            group[-1].start()
        copies += group
    first = 0
    stores = []
    for j, terms in enumerate(jobs):
        total = None
        for i, (_, _, _, turn) in enumerate(terms):
            copies[first + i].wait()
            value = term_buf[first + i].astype(F32)
            value = turn_chunks(value) if turn else value
            total = value if total is None else total + value
        first += len(terms)
        out_buf[j] = total.astype(BF16)
        stores.append(pltpu.make_async_copy(out_buf.at[j], outs[j], out_sems.at[j]))
        stores[-1].start()
    for store in stores:
        store.wait()


def sums(info, arrays, jobs):
    cols = arrays[0].shape[1]
    rows, terms = 128, sum(len(job) for job in jobs)
    return pl.pallas_call(
        functools.partial(sums_kernel, jobs, len(arrays)),
        grid_spec=pltpu.PrefetchScalarGridSpec(
            num_scalar_prefetch=1,
            grid=(1,),
            in_specs=[ANY] * len(arrays),
            out_specs=[ANY] * len(jobs),
            scratch_shapes=[
                pltpu.VMEM((terms, rows, cols), BF16),
                pltpu.VMEM((len(jobs), rows, cols), BF16),
                pltpu.SemaphoreType.DMA((terms,)),
                pltpu.SemaphoreType.DMA((len(jobs),)),
            ],
        ),
        out_shape=[shape_of((rows, cols), BF16)] * len(jobs),
        compiler_params=settings(1, 60),
        cost_estimate=cost(False),
        name="sums",
    )(info, *arrays)


def core_jobs(keep, came):
    return [[(a, far * 256, pick, False) for a in (keep, came)] for far in (0, 1) for pick in (0, 1)]


def core_sum_kernel(info, left_ref, right_ref, *outs):
    total = (left_ref[...].astype(F32) + right_ref[...].astype(F32)).astype(BF16)
    block = pl.program_id(1)
    place = block // 2 * 2 + jnp.bitwise_xor(block % 2, info[2])
    for i, out in enumerate(outs):

        @pl.when(place == i)
        def _():
            out[...] = total


def core_sum(info, keep, came):
    groups, rows, cols = keep.shape
    spec = pl.BlockSpec((1, rows // 4, cols), lambda g, i, info: (g, i, 0))
    return pl.pallas_call(
        core_sum_kernel,
        grid_spec=pltpu.PrefetchScalarGridSpec(
            num_scalar_prefetch=1,
            grid=(groups, 4),
            in_specs=[spec] * 2,
            out_specs=[pl.BlockSpec((1, rows // 4, cols), lambda g, i, info: (g, 0, 0))] * 4,
        ),
        out_shape=[shape_of((groups, rows // 4, cols), BF16)] * 4,
        compiler_params=settings(2, 24),
        cost_estimate=cost(False),
        name="core_sum",
    )(info, keep, came)


def weight_grad_kernel(nt_ref, back0_ref, back1_ref, gt_ref, att_ref, keep_ref, send_ref):
    cols = back0_ref.shape[2]
    part, block = pl.program_id(0), pl.program_id(1)

    def rows(target, back_ref):
        target[0, :, :cols] = dot(nt_ref[...], back_ref[0], 1, 0).astype(BF16)
        target[0, :, cols:] = dot(gt_ref[...], att_ref[0], 1, 0).astype(BF16)

    for j, back_ref in enumerate((back0_ref, back1_ref)):

        @pl.when((part == 0) & (block % 2 == j))
        def _():
            rows(send_ref, back_ref)

        @pl.when((part == 1) & (block % 2 == j))
        def _():
            rows(keep_ref, back_ref)


def weight_grad(normed_t, backs, grad_t, attended):
    width, tok = normed_t.shape
    cols, feats = backs[0].shape[2], attended.shape[2]
    half = pl.BlockSpec((width // 2, tok), lambda p, k: (1 - p, 0))
    side = pl.BlockSpec((1, tok, cols), lambda p, k: (k // 2, 0, 0))
    shape = (1, width // 2, cols + feats)
    return pl.pallas_call(
        weight_grad_kernel,
        grid=(2, 4),
        in_specs=[half, side, side, half, pl.BlockSpec((1, tok, feats), lambda p, k: (k, 0, 0))],
        out_specs=[
            pl.BlockSpec(shape, lambda p, k: (jnp.where(p == 0, 0, k), 0, 0)),
            pl.BlockSpec(shape, lambda p, k: (jnp.where(p == 0, k, 3), 0, 0)),
        ],
        out_shape=[shape_of((4, width // 2, cols + feats), BF16)] * 2,
        compiler_params=settings(2, 60),
        cost_estimate=cost(True),
        name="weight_grad",
    )(normed_t, *backs, grad_t, attended)


def after(value, *others):
    return lax.optimization_barrier((value,) + others)[0]


def per_device_rows(
    tokens,
    teacher,
    lengths,
    attn_gain,
    q_weight,
    k_weight,
    v_weight,
    q_gain,
    k_gain,
    o_weight,
    ffn_gain,
    gate_weight,
    up_weight,
    down_weight,
):
    z = lax.axis_index("tp")
    ctx = lax.axis_index("ctx")
    fsdp = lax.axis_index("fsdp")
    rows_dev, tok, width = tokens.shape
    quarter = width // 4
    hd = q_gain.shape[0] * 4
    q_cols, k_cols = q_weight.shape[1], k_weight.shape[1]
    proj = q_cols + 2 * k_cols
    heads = (q_cols // hd, k_cols // hd)
    units = gate_weight.shape[1]
    slots = rows_dev * 4 * tok * 2

    def x_swap(v):
        return lax.ppermute(v, "fsdp", X_SWAP)

    def core_swap(v):
        return lax.ppermute(v, "fsdp", CORE_SWAP)

    def y_swap(v):
        return lax.ppermute(v, "ctx", Y_SWAP)

    def z_up(v):
        return lax.ppermute(v, "tp", Z_UP)

    def z_far(v):
        return lax.ppermute(v, "tp", Z_FAR)

    def z_down(v):
        return lax.ppermute(v, "tp", Z_DOWN)

    def natural(v):
        v = jnp.concatenate([v[0:1], v[2:3], v[1:2], v[3:4]], axis=0)
        v = jnp.where(fsdp % 2 == 0, v, jnp.concatenate([v[1:2], v[0:1], v[3:4], v[2:3]], axis=0))
        return jnp.where(fsdp // 2 == 0, v, jnp.concatenate([v[2:4], v[0:2]], axis=0))

    v = {}

    def sync():
        v.update(lax.optimization_barrier(dict(v)))

    length = lax.dynamic_slice_in_dim(lengths, z, 1, 0)
    info = jnp.concatenate([jnp.stack([z, fsdp, ctx]).astype(jnp.int32), length])
    w_proj = join(q_weight, k_weight, v_weight)
    proj_z = [z_up(w_proj), z_far(w_proj), z_down(w_proj)]
    proj_own = jnp.concatenate([w_proj, x_swap(w_proj)], axis=0)
    count_here = jnp.sum(lengths).astype(F32)[None]
    vector = jnp.concatenate([attn_gain, ffn_gain, q_gain, k_gain]).astype(F32)
    vector = jnp.concatenate([vector, count_here, jnp.zeros((640 - 545,), F32)])[None]
    vector = jnp.concatenate([vector, x_swap(vector)], axis=0)
    vector = jnp.concatenate([vector, core_swap(vector)], axis=0)
    w_out, w_ffn, *w_chunks = pack(info, o_weight, gate_weight, up_weight, down_weight)
    pos = (ctx * tok + jnp.arange(tok, dtype=jnp.int32)).astype(F32)
    frequency = THETA ** (-(2.0 * jnp.arange(hd // 2, dtype=F32)) / hd)
    angles = frequency[:, None] * pos[None, :]
    head_gains = natural(vector[:, 2 * quarter : 544])
    v.update(
        info=info,
        proj_own=proj_own,
        proj_z=jnp.concatenate(proj_z, axis=0),
        w_out=w_out,
        w_ffn=w_ffn,
        w_chunks=w_chunks,
        gain_one=vector[:, :quarter].reshape(1, width),
        gain_two=vector[:, quarter : 2 * quarter].reshape(1, width),
        total_count=jnp.sum(vector[:, 544]),
        gain_q=head_gains[:, : hd // 4].reshape(hd, 1),
        gain_k=head_gains[:, hd // 4 :].reshape(hd, 1),
        cos_part=jnp.cos(angles),
        sin_part=jnp.sin(angles),
    )
    sync()
    info = v["info"]

    proj_zfar = x_swap(v["proj_z"])
    out_z = [z_up(v["w_out"]), z_far(v["w_out"]), z_down(v["w_out"])]
    own_core = core_swap(v["proj_own"])
    x_in, normed_one_t = norm_one(info, tokens, v["gain_one"], 256)
    v.update(
        proj_zfar=proj_zfar, own_core=own_core, x_in=x_in, normed_one_t=normed_one_t, out_z=out_z
    )
    sync()

    plan_proj = [[(0, 0), (0, quarter), (3, 0), (3, quarter)]]
    plan_proj += [[(p, k * quarter) for p in (1, 2, 4, 5)] for k in range(3)]
    weights_proj = [v["proj_own"], v["proj_z"], v["proj_zfar"], v["own_core"]]
    weights_proj += [core_swap(v["proj_z"]), core_swap(v["proj_zfar"])]
    one = [z_up(v["w_chunks"][0]), z_up(v["w_chunks"][3])]
    ffn_far = x_swap(v["w_ffn"])
    tables = [v[name] for name in ("cos_part", "sin_part", "gain_q", "gain_k")]

    def make(block, *then):
        normed_t = after(v["normed_one_t"], *then)
        return project(info, (plan_proj, weights_proj), normed_t, *tables, heads, block)

    theirs = [make(lambda s: 2 * (1 - s[2]))]
    got = [y_swap(theirs[0][0])]
    theirs.append(make(lambda s: 2 * (1 - s[2]) + 1, theirs[0][0]))
    got.append(y_swap(theirs[1][0]))
    mine = [make(lambda s: 2 * s[2], theirs[1][0])]
    mine.append(make(lambda s: 2 * s[2] + 1, mine[0][0]))
    v.update(
        one=one,
        ffn_far=ffn_far,
        weights_proj=weights_proj,
        mine=mine,
        theirs=theirs,
        got0=got[0],
    )
    sync()

    one_far = [x_swap(v["one"][0])]
    three = [z_down(v["w_chunks"][0])]
    own_cores = [core_swap(v["w_ffn"]), core_swap(v["ffn_far"])]
    first = attn_fwd(info, v["mine"][0][0], v["got0"], hd)
    v.update(first=first, got1=got[1], one_far=one_far, three=three, own_cores=own_cores)
    sync()

    arrived = [y_swap(v["first"][1])]
    three = v["three"] + [z_down(v["w_chunks"][1])]
    out_blocks = jnp.concatenate([v["w_out"]] + v["out_z"], axis=0)
    out_far = x_swap(out_blocks)
    one_cores = [core_swap(v["one"][0]), core_swap(v["one_far"][0])]
    second = attn_fwd(info, v["mine"][1][0], v["got1"], hd)
    v.update(
        second=second,
        arrived=arrived,
        three=three,
        out_blocks=out_blocks,
        out_far=out_far,
        one_cores=one_cores,
    )
    sync()

    arrived = v["arrived"] + [y_swap(v["second"][1])]
    three = v["three"] + [z_down(v["w_chunks"][2])]
    one_far = v["one_far"] + [x_swap(v["one"][1][:, :units])]
    weights_out = [v["out_blocks"], v["out_far"]]
    weights_out += [core_swap(v["out_blocks"]), core_swap(v["out_far"])]
    v.update(arrived=arrived, three=three, one_far=one_far, weights_out=weights_out)
    sync()

    plan_out = [[(p, k * quarter) for p in range(4)] for k in range(4)]
    two = [z_up(v["one"][0])]
    three_far = [x_swap(v["three"][0])]
    one_far = v["one_far"] + [y_swap(v["one_far"][0])]
    one_cores = v["one_cores"] + [core_swap(v["one"][1]), core_swap(v["one_far"][1])]
    resid, normed_two, normed_two_t, attended = out_proj(
        info,
        v["x_in"],
        [v["first"][0], v["second"][0]],
        v["arrived"],
        (plan_out, v["weights_out"]),
        v["gain_two"],
        256,
    )
    v.update(
        two=two,
        three_far=three_far,
        one_far=one_far,
        one_cores=one_cores,
        resid=resid,
        normed_two=normed_two,
        normed_two_t=normed_two_t,
        attended=attended,
    )
    sync()

    plan0 = [[(i, 0, j * units) for j in range(3)] for i in range(4)]
    plan_mixed = [[(0, 0, 0), (1, 0, 0), (1, 0, units)], [(i, 0, 0) for i in (2, 3, 4)]]
    plan_mixed += [[(5, 0, 0), (6, 0, 0), (6, 0, units)], [(i, 0, 0) for i in (7, 8, 9)]]
    scale = (slots / v["total_count"])[None]
    weights0 = [v["w_ffn"], v["ffn_far"]] + v["own_cores"]
    c0, cf, c1, cb = v["one_cores"]
    weights1 = v["one"] + v["one_far"] + [c0, c1, cf, cb, core_swap(v["one_far"][2])]
    two = v["two"] + [z_up(v["one"][1])]
    three_far = v["three_far"] + [x_swap(v["three"][1]), y_swap(v["three_far"][0])]
    two_far = [x_swap(v["two"][0])]
    three_cores = [core_swap(v["three"][0])]
    acts_a, hiddens_a, sum_a = ffn_fwd(
        info,
        scale,
        v["normed_two"],
        v["resid"],
        None,
        [(plan0, weights0), (plan_mixed, weights1)],
        units,
        256,
    )
    v.update(
        scale=scale,
        weights0=weights0,
        weights1=weights1,
        two=two,
        three_far=three_far,
        two_far=two_far,
        three_cores=three_cores,
        acts_a=acts_a,
        hiddens_a=hiddens_a,
        sum_a=sum_a,
    )
    sync()

    plan_chunks = [[(3 * p + j, 0, 0) for j in range(3)] for p in range(4)]
    weights3 = v["three"] + v["three_far"] + v["three_cores"]
    weights3 += [core_swap(part) for part in v["three"][1:]]
    weights3 += [core_swap(part) for part in v["three_far"]]
    two_far = v["two_far"] + [x_swap(v["two"][1][:, :units]), y_swap(v["two_far"][0])]
    two_cores = [core_swap(part) for part in v["two"] + v["two_far"]]
    acts_b, hiddens_b, sum_b = ffn_fwd(
        info, v["scale"], v["normed_two"], v["sum_a"], None, [(plan_chunks, weights3)], units, 256
    )
    v.update(
        weights3=weights3,
        two_far=two_far,
        two_cores=two_cores,
        acts_b=acts_b,
        hiddens_b=hiddens_b,
        sum_b=sum_b,
    )
    sync()

    weights2 = v["two"] + v["two_far"] + v["two_cores"]
    weights2 += [core_swap(part) for part in v["two_far"][1:]]
    acts_c, hiddens_c, result_low, grad_result, grad_low, grad_low_t, square = ffn_fwd(
        info, v["scale"], v["normed_two"], v["sum_b"], teacher, [(plan_mixed, weights2)], units, 256
    )
    v.update(
        weights2=weights2,
        acts_c=acts_c,
        hiddens_c=hiddens_c,
        result_low=result_low,
        grad_result=grad_result,
        grad_low=grad_low,
        grad_low_t=grad_low_t,
        square=square,
    )
    sync()

    def ffn_back(plan, weights, acts, hiddens, block, total):
        return ffn_bwd(
            v["grad_low"],
            (v[acts], v[hiddens], block),
            (plan, v[weights]),
            total,
            v["normed_two_t"],
            v["grad_low_t"],
            256,
        )

    turned = [False, False, True]
    output = lax.all_gather(v["result_low"], "tp", axis=0, tiled=False)
    total, keep2, send2 = ffn_back(plan_mixed, "weights2", "acts_c", "hiddens_c", 0, None)
    v.update(total=total, keep2=keep2, send2=send2)
    sync()

    came2 = core_swap(v["send2"])
    total, keep1, send1 = ffn_back(plan_mixed, "weights1", "acts_a", "hiddens_a", 1, v["total"])
    v.update(came2=came2, total=total, keep1=keep1, send1=send1)
    sync()

    came1 = core_swap(v["send1"])
    sum2 = sums(info, [v["keep2"], v["came2"]], core_jobs(0, 1))
    far_t2 = x_swap(sum2[3])
    total, keep3, send3 = ffn_back(
        plan_chunks, "weights3", "acts_b", "hiddens_b", 0, after(v["total"], sum2[0])
    )
    v.update(
        came1=came1,
        sum2=sum2,
        far_t2=far_t2,
        total=total,
        keep3=keep3,
        send3=send3,
    )
    sync()

    came3 = core_swap(v["send3"])
    far_h2 = x_swap(v["sum2"][2])
    there2, *sum1 = sums(
        info,
        [v["sum2"][1], v["far_t2"], v["keep1"], v["came1"]],
        [[(0, 0, None, False), (1, 0, None, False)]] + core_jobs(2, 3),
    )
    there2 = y_swap(there2)
    total, keep0, send0 = ffn_back(
        plan0, "weights0", "acts_a", "hiddens_a", 0, after(v["total"], sum1[0])
    )
    v.update(
        came3=came3,
        far_h2=far_h2,
        there2=there2,
        sum1=sum1,
        total=total,
        keep0=keep0,
        send0=send0,
    )
    sync()

    came0 = core_swap(v["send0"])
    far_t1 = x_swap(v["sum1"][3])
    plane = [(0, 0, None, False), (1, 0, None, False), (2, 0, None, True)]
    part2, *sum3 = sums(
        info,
        [v["sum2"][0], v["far_h2"], v["there2"], v["keep3"], v["came3"]],
        [plane] + core_jobs(3, 4),
    )
    down2 = z_down(part2)
    grad_resid, grad_attn_t, a0, a1, b0, b1, gain_two_sum = norm_two_back(
        info,
        after(v["total"], sum3[0]),
        v["resid"],
        v["grad_result"],
        v["gain_two"],
        (plan_out, v["weights_out"]),
        256,
    )
    grad_got = [y_swap(b0), y_swap(b1)]
    v.update(
        came0=came0,
        far_t1=far_t1,
        sum3=sum3,
        grad_resid=grad_resid,
        grad_attn_t=grad_attn_t,
        grad_mine=[a0, a1],
        gain_two_sum=gain_two_sum,
        grad_got0=grad_got[0],
    )
    sync()

    def attn_back(j, grad):
        out, got_ref = v["first" if j == 0 else "second"], v[f"got{j}"]
        return attn_bwd(
            info, v["mine"][j][0], got_ref, out[0], out[1], grad, v[f"grad_got{j}"], out[2], hd
        )

    far_h1 = x_swap(v["sum1"][2])
    there1, *sum0 = sums(
        info,
        [v["sum1"][1], v["far_t1"], v["keep0"], v["came0"]],
        [[(0, 0, None, False), (1, 0, None, False)]] + core_jobs(2, 3),
    )
    there1 = y_swap(there1)
    far_t3 = x_swap(v["sum3"][3])
    back0 = attn_back(0, after(v["grad_mine"][0], sum0[0]))
    v.update(
        far_h1=far_h1,
        there1=there1,
        far_t3=far_t3,
        down2=down2,
        sum0=sum0,
        back0=back0,
        grad_got1=grad_got[1],
    )
    sync()

    heads0 = y_swap(v["back0"][1])
    far_h3 = x_swap(v["sum3"][2])
    far_t0 = x_swap(v["sum0"][3])
    there3, two_down = sums(
        info,
        [v["sum3"][1], v["far_t3"], v["sum1"][0], v["far_h1"], v["there1"], v["down2"]],
        [
            [(0, 0, None, False), (1, 0, None, False)],
            [(2, 0, None, False), (3, 0, None, False), (4, 0, None, True), (5, 0, None, False)],
        ],
    )
    there3_got = y_swap(there3)
    two_down_got = z_down(two_down)
    back1 = attn_back(1, after(v["grad_mine"][1], there3, two_down, output))
    v.update(
        heads0=heads0, far_h3=far_h3, far_t0=far_t0, there3=there3_got, back1=back1
    )
    sync()

    heads1 = y_swap(v["back1"][1])
    far_h0 = x_swap(v["sum0"][2])
    part3, there0 = sums(
        info,
        [v["sum3"][0], v["far_h3"], v["there3"], v["sum0"][1], v["far_t0"]],
        [plane, [(3, 0, None, False), (4, 0, None, False)]],
    )
    up3 = z_up(part3)
    tables = [v[name] for name in ("cos_part", "sin_part", "gain_q", "gain_k")]
    head0 = head_back(
        info, v["back0"][0], v["heads0"], v["mine"][0][1], v["theirs"][0][1], *tables, heads
    )
    v.update(heads1=heads1, head0=head0, there0=there0)
    sync()

    there0 = y_swap(v["there0"])
    head1 = head_back(
        info, v["back1"][0], v["heads1"], v["mine"][1][1], v["theirs"][1][1], *tables, heads
    )
    def last_norm(part, *then):
        return norm_one_back(
            info,
            [v["head0"][0], after(head1[0], *then)],
            (plan_proj, v["weights_proj"]),
            v["x_in"],
            v["grad_resid"],
            v["gain_one"],
            tok // 4,
            part,
        )

    low_first, gain_first = last_norm(0)
    low_second, gain_second = last_norm(1, low_first)
    gathered = [lax.all_gather(low_first, "tp", axis=0, tiled=False)]
    tokens_low, gain_one_sum = low_second, gain_first + gain_second
    v.update(head1=head1, tokens_low=tokens_low, gain_one_sum=gain_one_sum, up3=up3)
    v.update(there0=there0, far_h0=far_h0, two_down=two_down_got)
    sync()

    gathered.append(lax.all_gather(v["tokens_low"], "tp", axis=0, tiled=False))
    keep, send = weight_grad(
        v["normed_one_t"], [v["head0"][0], v["head1"][0]], v["grad_attn_t"], v["attended"]
    )
    gain_heads = v["head0"][1] + v["head1"][1]
    vector = jnp.concatenate(
        [
            natural(v["gain_one_sum"].reshape(4, quarter)).reshape(1, width),
            natural(v["gain_two_sum"].reshape(4, quarter)).reshape(1, width),
            gain_heads[:, 0].reshape(1, hd),
            gain_heads[:, 1].reshape(1, hd),
            jnp.sum(v["square"]).reshape(1, 1),
            jnp.zeros((1, 127), F32),
        ],
        axis=1,
    )
    vector = vector + core_swap(vector)
    v.update(keep=keep, send=send)
    v.update(vector=vector)
    sync()

    rows = quarter // 2
    flat = lambda a: a.reshape(4 * rows, a.shape[-1])
    attn_sums = [flat(p) for p in core_sum(info, v["keep"], core_swap(v["send"]))]
    vector = v["vector"] + x_swap(v["vector"])
    v.update(sums=attn_sums, vector=vector)
    sync()

    far_t = x_swap(v["sums"][3])
    part0 = summed([v["sum0"][0], v["far_h0"], v["there0"]], turned)
    ffn_sum = summed([part0, v["two_down"], v["up3"]], None, F32)
    vector = v["vector"] + y_swap(v["vector"])
    v.update(far_t=far_t, ffn_sum=ffn_sum, vector=vector)
    sync()

    far_h = x_swap(v["sums"][2])
    there = y_swap(summed([v["sums"][1], v["far_t"]]))
    v.update(far_h=far_h, there=there)
    sync()

    parts = summed([v["sums"][0], v["far_h"], v["there"]])
    parts = [parts[k * rows : (k + 1) * rows] for k in range(4)]
    parts = [parts[0], z_down(parts[1]), z_far(parts[2]), z_up(parts[3])]
    ffn_other = y_swap(v["ffn_sum"])
    v.update(parts=parts)
    sync()

    attn_sum = summed(v["parts"], None, F32)
    vector = v["vector"] + lax.ppermute(v["vector"], "tp", Z_NEAR)
    v.update(attn_sum=attn_sum, vector=vector)
    v.update(ffn_other=ffn_other)
    sync()

    def finish(own, other):
        return jnp.concatenate(
            [jnp.where(ctx == 0, own, other), jnp.where(ctx == 0, other, own)], axis=0
        )

    def columns(first):
        parts = [ffn_grad[:, first(j) : first(j) + third] for j in range(3)]
        return jnp.concatenate(
            [
                jnp.where(ctx == 0, parts[0], parts[2]),
                parts[1],
                jnp.where(ctx == 0, parts[2], parts[0]),
            ],
            axis=1,
        )

    attn_other = y_swap(v["attn_sum"])
    vector = v["vector"] + lax.ppermute(v["vector"], "tp", Z_FAR)
    third = units // 3
    ffn_grad = finish(v["ffn_sum"], turn_chunks(v["ffn_other"]))
    grad_gate = columns(lambda j: 2 * j * third)
    grad_up = columns(lambda j: (2 * j + 1) * third)
    grad_down = columns(lambda j: 2 * units + j * third).T
    grad = jnp.zeros((rows_dev, tok, width), F32)
    grad = lax.dynamic_update_slice(grad, gathered[0].astype(F32), (0, 0, 0))
    v.update(vector=vector, attn_other=attn_other, grad=grad)
    v.update(grad_gate=grad_gate, grad_up=grad_up, grad_down=grad_down)
    sync()

    tokens_grad = lax.dynamic_update_slice(v["grad"], gathered[1].astype(F32), (0, tok // 2, 0))
    sums_all = v["vector"][0]

    attn_grad = finish(v["attn_sum"], v["attn_other"])
    teacher_loss = sums_all[2 * width + 2 * hd] / (v["total_count"] * width)

    def own_part(at, size):
        return lax.dynamic_slice_in_dim(sums_all, at + fsdp * (size // 4), size // 4, 0)

    return (
        output,
        teacher_loss,
        tokens_grad,
        own_part(0, width),
        attn_grad[:, :q_cols],
        attn_grad[:, q_cols : q_cols + k_cols],
        attn_grad[:, q_cols + k_cols : proj],
        own_part(2 * width, hd),
        own_part(2 * width + hd, hd),
        attn_grad[:, proj:].T,
        own_part(width, width),
        v["grad_gate"],
        v["grad_up"],
        v["grad_down"],
    )


def solution(mesh):
    return jax.shard_map(
        per_device_rows if fits(mesh) else per_device_any,
        mesh=mesh,
        in_specs=(
            P("fsdp", "ctx", None),
            P("fsdp", "ctx", None),
            P("fsdp"),
            P("fsdp"),
            P("fsdp", "tp"),
            P("fsdp", "tp"),
            P("fsdp", "tp"),
            P("fsdp"),
            P("fsdp"),
            P("tp", "fsdp"),
            P("fsdp"),
            P("fsdp", "tp"),
            P("fsdp", "tp"),
            P("tp", "fsdp"),
        ),
        out_specs=(
            P("fsdp", "ctx", None),
            P(),
            P("fsdp", "ctx", None),
            P("fsdp"),
            P("fsdp", "tp"),
            P("fsdp", "tp"),
            P("fsdp", "tp"),
            P("fsdp"),
            P("fsdp"),
            P("tp", "fsdp"),
            P("fsdp"),
            P("fsdp", "tp"),
            P("fsdp", "tp"),
            P("tp", "fsdp"),
        ),
        check_vma=False,
    )
```

```python
import functools
import math

import jax
import jax.numpy as jnp
from jax import lax
from jax.experimental import pallas as pl
from jax.experimental.pallas import tpu as pltpu
from jax.sharding import PartitionSpec as P

EPS = 1e-05
THETA = 1000000.0
NEGATIVE = -1e30


def rms_scale(field_in, gain_vec):
    return (
        field_in * lax.rsqrt(jnp.mean(field_in * field_in, axis=-1, keepdims=True) + EPS) * gain_vec
    )


def rotate(field_in, positions):
    half_dim = field_in.shape[-1] // 2
    frequency = THETA ** (-(2.0 * jnp.arange(half_dim, dtype=jnp.float32)) / field_in.shape[-1])
    angles = positions[:, None] * frequency[None, :]
    cos_part = jnp.cos(angles)[:, None, :]
    sin_part = jnp.sin(angles)[:, None, :]
    lower_half = field_in[..., :half_dim]
    upper_half = field_in[..., half_dim:]
    return jnp.concatenate(
        [
            lower_half * cos_part - upper_half * sin_part,
            upper_half * cos_part + lower_half * sin_part,
        ],
        axis=-1,
    )


def linear(left_mat, right_mat):
    return jnp.dot(left_mat, right_mat, preferred_element_type=jnp.float32)


def linear_left(left_mat, right_mat):
    return lax.dot_general(
        left_mat, right_mat, (((0,), (0,)), ((), ())), preferred_element_type=jnp.float32
    )


def linear_right(left_mat, right_mat):
    return lax.dot_general(
        left_mat, right_mat, (((1,), (1,)), ((), ())), preferred_element_type=jnp.float32
    )


def swiglu(gate_act, up_act):
    return jax.nn.silu(gate_act) * up_act


def per_device_any(
    tokens,
    teacher,
    lengths,
    attn_gain,
    q_weight,
    k_weight,
    v_weight,
    q_gain,
    k_gain,
    o_weight,
    ffn_gain,
    gate_weight,
    up_weight,
    down_weight,
):
    (
        gain_one,
        w_query,
        w_key,
        w_value,
        gain_query,
        gain_key,
        w_output,
        gain_two,
        w_gate,
        w_upper,
        w_down,
    ) = (
        lax.all_gather(attn_gain, "fsdp", axis=0, tiled=True),
        lax.all_gather(q_weight, "fsdp", axis=0, tiled=True),
        lax.all_gather(k_weight, "fsdp", axis=0, tiled=True),
        lax.all_gather(v_weight, "fsdp", axis=0, tiled=True),
        lax.all_gather(q_gain, "fsdp", axis=0, tiled=True),
        lax.all_gather(k_gain, "fsdp", axis=0, tiled=True),
        lax.all_gather(o_weight, "fsdp", axis=1, tiled=True),
        lax.all_gather(ffn_gain, "fsdp", axis=0, tiled=True),
        lax.all_gather(gate_weight, "fsdp", axis=0, tiled=True),
        lax.all_gather(up_weight, "fsdp", axis=0, tiled=True),
        lax.all_gather(down_weight, "fsdp", axis=1, tiled=True),
    )
    rows_dev, block_len, model_width = tokens.shape
    count_tok = rows_dev * block_len
    head_dim = gain_query.shape[0]
    q_heads = w_query.shape[1] // head_dim
    kv_heads = w_key.shape[1] // head_dim
    group_size = q_heads // kv_heads
    score_scale = head_dim ** (-0.5)
    row_len = block_len * lax.axis_size("ctx")
    key_block = math.gcd(row_len, 512)
    block_start = lax.axis_index("ctx") * block_len
    tiles_used = (block_start + block_len + key_block - 1) // key_block
    slot_pos = block_start + jnp.arange(block_len, dtype=jnp.int32)
    positions = slot_pos.astype(jnp.float32)
    valid = (slot_pos[None, :] < lengths[:, None]).astype(jnp.float32)
    slots = count_tok * lax.axis_size("fsdp") * lax.axis_size("ctx")
    gain_two_f = gain_two.astype(jnp.float32)
    gain_one_f = gain_one.astype(jnp.float32)
    inputs = tokens.astype(jnp.float32)
    normed_one, back_one = jax.vjp(rms_scale, inputs, gain_one_f)
    normed_low = normed_one.astype(jnp.bfloat16).reshape(count_tok, model_width)
    query_raw = linear(normed_low, w_query)
    key_raw = linear(normed_low, w_key)
    value_raw = linear(normed_low, w_value)

    def heads_post(raw_heads, gain_vec):
        shaped = raw_heads.reshape(rows_dev, block_len, -1, head_dim)
        return rotate(rms_scale(shaped, gain_vec), positions)

    query_rot, query_back = jax.vjp(heads_post, query_raw, gain_query.astype(jnp.float32))
    key_rot, key_back = jax.vjp(heads_post, key_raw, gain_key.astype(jnp.float32))
    queries = query_rot.astype(jnp.bfloat16).reshape(
        rows_dev, block_len, kv_heads, group_size, head_dim
    )
    key_rows = key_rot.astype(jnp.bfloat16).reshape(rows_dev, block_len, kv_heads * head_dim)
    values = value_raw.astype(jnp.bfloat16).reshape(rows_dev, block_len, kv_heads * head_dim)
    keys_all, values_all = (
        lax.all_gather(key_rows, "ctx", axis=1, tiled=True),
        lax.all_gather(values, "ctx", axis=1, tiled=True),
    )

    def key_tile(tile_index):
        tile_start = tile_index * key_block
        key_pos = tile_start + jnp.arange(key_block, dtype=jnp.int32)
        key_part = lax.dynamic_slice_in_dim(keys_all, tile_start, key_block, 1).reshape(
            rows_dev, key_block, kv_heads, head_dim
        )
        value_part = lax.dynamic_slice_in_dim(values_all, tile_start, key_block, 1).reshape(
            rows_dev, key_block, kv_heads, head_dim
        )
        scores = (
            jnp.einsum("rqhgd,rkhd->rhgqk", queries, key_part, preferred_element_type=jnp.float32)
            * score_scale
        )
        allowed = (key_pos[None, None, :] <= slot_pos[None, :, None]) & (
            key_pos[None, None, :] < lengths[:, None, None]
        )
        return (tile_start, scores, allowed[:, None, None], key_part, value_part)

    stat_shape = (rows_dev, kv_heads, group_size, block_len)

    def stats_step(tile_index, carried):
        running_max, running_sum = carried
        tile_start, scores, allowed, key_part, value_part = key_tile(tile_index)
        masked = jnp.where(allowed, scores, NEGATIVE)
        new_max = jnp.maximum(running_max, jnp.max(masked, axis=-1))
        terms = jnp.where(allowed, jnp.exp(masked - new_max[..., None]), 0.0)
        return (new_max, running_sum * jnp.exp(running_max - new_max) + jnp.sum(terms, axis=-1))

    running_max, running_sum = lax.fori_loop(
        0,
        tiles_used,
        stats_step,
        (jnp.full(stat_shape, NEGATIVE, jnp.float32), jnp.zeros(stat_shape, jnp.float32)),
    )
    log_total = running_max + jnp.log(running_sum)
    out_shape = (rows_dev, block_len, kv_heads, group_size, head_dim)

    def value_step(tile_index, carried):
        rounded_out, exact_out = carried
        tile_start, scores, allowed, key_part, value_part = key_tile(tile_index)
        tile_probs = jnp.where(allowed, jnp.exp(scores - log_total[..., None]), 0.0)
        rounded_out = rounded_out + jnp.einsum(
            "rhgqk,rkhd->rqhgd",
            tile_probs.astype(jnp.bfloat16),
            value_part,
            preferred_element_type=jnp.float32,
        )
        exact_out = exact_out + jnp.einsum(
            "rhgqk,rkhd->rqhgd", tile_probs, value_part.astype(jnp.float32)
        )
        return (rounded_out, exact_out)

    rounded_out, exact_out = lax.fori_loop(
        0,
        tiles_used,
        value_step,
        (jnp.zeros(out_shape, jnp.float32), jnp.zeros(out_shape, jnp.float32)),
    )
    attended = rounded_out.astype(jnp.bfloat16).reshape(count_tok, q_heads * head_dim)
    attn_total = lax.psum(linear(attended, w_output), "tp")
    resid = inputs + attn_total.reshape(rows_dev, block_len, model_width)
    normed_two, back_two = jax.vjp(rms_scale, resid, gain_two_f)
    normed_second = normed_two.astype(jnp.bfloat16).reshape(count_tok, model_width)
    gate_act = linear(normed_second, w_gate)
    up_act = linear(normed_second, w_upper)
    hidden_full, back_glu = jax.vjp(swiglu, gate_act, up_act)
    hidden = hidden_full.astype(jnp.bfloat16)
    ffn_total = lax.psum(linear(hidden, w_down), "tp")
    result = resid + ffn_total.reshape(rows_dev, block_len, model_width)
    error_value = result - teacher.astype(jnp.float32)
    valid_col = valid[..., None]
    total_square, total_count = lax.psum(
        (jnp.sum(valid_col * error_value * error_value), jnp.sum(valid)), ("fsdp", "ctx")
    )
    teacher_loss = total_square / (total_count * model_width)
    grad_result = valid_col * error_value * (slots / total_count)
    grad_low = grad_result.astype(jnp.bfloat16).reshape(count_tok, model_width)
    grad_down = linear_left(hidden, grad_low)
    grad_hidden = linear_right(grad_low, w_down)
    grad_gate_full, grad_up_full = back_glu(grad_hidden)
    grad_gate = grad_gate_full.astype(jnp.bfloat16)
    grad_up = grad_up_full.astype(jnp.bfloat16)
    grad_wgate = linear_left(normed_second, grad_gate)
    grad_wup = linear_left(normed_second, grad_up)
    normed_two_part = linear_right(grad_gate, w_gate) + linear_right(grad_up, w_upper)
    grad_normed_two = lax.psum(normed_two_part, "tp")
    grad_resid_norm, grad_gain_two = back_two(
        grad_normed_two.reshape(rows_dev, block_len, model_width)
    )
    grad_resid = grad_result + grad_resid_norm
    grad_attn_low = grad_resid.astype(jnp.bfloat16).reshape(count_tok, model_width)
    grad_woutput = linear_left(attended, grad_attn_low)
    grad_attended = linear_right(grad_attn_low, w_output).astype(jnp.bfloat16).reshape(out_shape)
    delta = jnp.einsum("rqhgd,rqhgd->rhgq", grad_attended.astype(jnp.float32), exact_out)
    full_shape = (rows_dev, row_len, kv_heads * head_dim)

    def grad_step(tile_index, carried):
        grad_queries, grad_keys, grad_values = carried
        tile_start, scores, allowed, key_part, value_part = key_tile(tile_index)
        tile_probs = jnp.where(allowed, jnp.exp(scores - log_total[..., None]), 0.0)
        grad_probs = jnp.einsum(
            "rqhgd,rkhd->rhgqk", grad_attended, value_part, preferred_element_type=jnp.float32
        )
        grad_scores = (tile_probs * (grad_probs - delta[..., None])).astype(jnp.bfloat16)
        grad_queries = (
            grad_queries
            + jnp.einsum(
                "rhgqk,rkhd->rqhgd", grad_scores, key_part, preferred_element_type=jnp.float32
            )
            * score_scale
        )
        key_term = (
            jnp.einsum(
                "rhgqk,rqhgd->rkhd", grad_scores, queries, preferred_element_type=jnp.float32
            )
            * score_scale
        )
        value_term = jnp.einsum(
            "rhgqk,rqhgd->rkhd",
            tile_probs.astype(jnp.bfloat16),
            grad_attended,
            preferred_element_type=jnp.float32,
        )
        grad_keys = lax.dynamic_update_slice_in_dim(
            grad_keys, key_term.reshape(rows_dev, key_block, kv_heads * head_dim), tile_start, 1
        )
        grad_values = lax.dynamic_update_slice_in_dim(
            grad_values, value_term.reshape(rows_dev, key_block, kv_heads * head_dim), tile_start, 1
        )
        return (grad_queries, grad_keys, grad_values)

    grad_queries, grad_keys, grad_values = lax.fori_loop(
        0,
        tiles_used,
        grad_step,
        (
            jnp.zeros(out_shape, jnp.float32),
            jnp.zeros(full_shape, jnp.float32),
            jnp.zeros(full_shape, jnp.float32),
        ),
    )
    key_grad, value_grad = (
        lax.psum_scatter(grad_keys, "ctx", scatter_dimension=1, tiled=True),
        lax.psum_scatter(grad_values, "ctx", scatter_dimension=1, tiled=True),
    )
    grad_query_raw, grad_gain_query = query_back(
        grad_queries.reshape(rows_dev, block_len, q_heads, head_dim)
    )
    grad_key_raw, grad_gain_key = key_back(
        key_grad.reshape(rows_dev, block_len, kv_heads, head_dim)
    )
    query_low = grad_query_raw.astype(jnp.bfloat16)
    key_low = grad_key_raw.astype(jnp.bfloat16)
    value_low = value_grad.reshape(count_tok, kv_heads * head_dim).astype(jnp.bfloat16)
    grad_wquery = linear_left(normed_low, query_low)
    grad_wkey = linear_left(normed_low, key_low)
    grad_wvalue = linear_left(normed_low, value_low)
    normed_part = (
        linear_right(query_low, w_query)
        + linear_right(key_low, w_key)
        + linear_right(value_low, w_value)
    )
    grad_normed_one, grad_gain_query, grad_gain_key = lax.psum(
        (normed_part, grad_gain_query, grad_gain_key), "tp"
    )
    grad_input_norm, grad_gain_one = back_one(
        grad_normed_one.reshape(rows_dev, block_len, model_width)
    )
    tokens_grad = grad_resid + grad_input_norm
    partials = (
        grad_gain_one,
        grad_wquery,
        grad_wkey,
        grad_wvalue,
        grad_gain_query,
        grad_gain_key,
        grad_woutput,
        grad_gain_two,
        grad_wgate,
        grad_wup,
        grad_down,
    )
    pieces = (
        lax.psum_scatter(partials[0], ("fsdp", "ctx"), scatter_dimension=0, tiled=True),
        lax.psum_scatter(partials[1], ("fsdp", "ctx"), scatter_dimension=0, tiled=True),
        lax.psum_scatter(partials[2], ("fsdp", "ctx"), scatter_dimension=0, tiled=True),
        lax.psum_scatter(partials[3], ("fsdp", "ctx"), scatter_dimension=0, tiled=True),
        lax.psum_scatter(partials[4], ("fsdp", "ctx"), scatter_dimension=0, tiled=True),
        lax.psum_scatter(partials[5], ("fsdp", "ctx"), scatter_dimension=0, tiled=True),
        lax.psum_scatter(partials[6], ("fsdp", "ctx"), scatter_dimension=1, tiled=True),
        lax.psum_scatter(partials[7], ("fsdp", "ctx"), scatter_dimension=0, tiled=True),
        lax.psum_scatter(partials[8], ("fsdp", "ctx"), scatter_dimension=0, tiled=True),
        lax.psum_scatter(partials[9], ("fsdp", "ctx"), scatter_dimension=0, tiled=True),
        lax.psum_scatter(partials[10], ("fsdp", "ctx"), scatter_dimension=1, tiled=True),
    )
    summed = (
        lax.all_gather(pieces[0], "ctx", axis=0, tiled=True),
        lax.all_gather(pieces[1], "ctx", axis=0, tiled=True),
        lax.all_gather(pieces[2], "ctx", axis=0, tiled=True),
        lax.all_gather(pieces[3], "ctx", axis=0, tiled=True),
        lax.all_gather(pieces[4], "ctx", axis=0, tiled=True),
        lax.all_gather(pieces[5], "ctx", axis=0, tiled=True),
        lax.all_gather(pieces[6], "ctx", axis=1, tiled=True),
        lax.all_gather(pieces[7], "ctx", axis=0, tiled=True),
        lax.all_gather(pieces[8], "ctx", axis=0, tiled=True),
        lax.all_gather(pieces[9], "ctx", axis=0, tiled=True),
        lax.all_gather(pieces[10], "ctx", axis=1, tiled=True),
    )
    return (
        result.astype(jnp.bfloat16),
        teacher_loss,
        tokens_grad,
        summed[0],
        summed[1],
        summed[2],
        summed[3],
        summed[4],
        summed[5],
        summed[6],
        summed[7],
        summed[8],
        summed[9],
        summed[10],
    )


BF16 = jnp.bfloat16
F32 = jnp.float32
LOG2E = math.log2(math.e)
X_SWAP = [(0, 2), (2, 0), (1, 3), (3, 1)]
CORE_SWAP = [(0, 1), (1, 0), (2, 3), (3, 2)]
Y_SWAP = [(0, 1), (1, 0)]
Z_UP = [(0, 1), (1, 2), (2, 3), (3, 0)]
Z_DOWN = [(0, 3), (1, 0), (2, 1), (3, 2)]
Z_NEAR = [(0, 1), (1, 0), (2, 3), (3, 2)]
Z_FAR = [(0, 2), (2, 0), (1, 3), (3, 1)]
MASKS = (0, 2, 1, 3)
ANY = pl.BlockSpec(memory_space=pl.ANY)
SMEM = pl.BlockSpec(memory_space=pltpu.SMEM)


def fits(mesh):
    return dict(mesh.shape) == {"fsdp": 4, "ctx": 2, "tp": 4}


def dot(left, right, left_dim, right_dim):
    return lax.dot_general(
        left, right, (((left_dim,), (right_dim,)), ((), ())), preferred_element_type=F32
    )


def sigmoid(v):
    return 0.5 * jnp.tanh(0.5 * v) + 0.5


def whole(shape):
    zeros = (0,) * len(shape)
    return pl.BlockSpec(shape, lambda *_: zeros, pipeline_mode=pl.Buffered(1))


def settings(dims, mib):
    return pltpu.CompilerParams(
        dimension_semantics=("arbitrary",) * dims, vmem_limit_bytes=mib << 20
    )


def shape_of(shape, dtype):
    return jax.ShapeDtypeStruct(shape, dtype)


def cost(large, microseconds=None):
    size = 1 << 42 if large else 1 << 10
    if microseconds is not None:
        size = int(microseconds * 1.15e9)
    return pl.CostEstimate(flops=size, bytes_accessed=size >> 12, transcendentals=0)


def pack_kernel(info, o_in, g_in, u_in, d_in, *refs):
    out_ref, ffn_ref, *chunk_refs, others_ref, o_ref, g_ref, u_ref, d_ref, sems = refs
    ctx = info[2]
    pairs = ((o_in, o_ref), (g_in, g_ref), (u_in, u_ref), (d_in, d_ref))
    copies = [pltpu.make_async_copy(a, b, sems.at[i]) for i, (a, b) in enumerate(pairs)]
    for copy in copies:
        copy.start()
    for copy in copies:
        copy.wait()
    out_ref[...] = o_ref[...].astype(F32).T.astype(BF16)
    third = g_ref.shape[1] // 3
    for j in range(3):
        at = pl.multiple_of(jnp.where(ctx == 0, j, 2 - j) * third, third)
        parts = [
            g_ref[:, pl.ds(at, third)],
            u_ref[:, pl.ds(at, third)],
            d_ref[pl.ds(at, third), :].astype(F32).T.astype(BF16),
        ]
        for i, part in enumerate(parts):
            chunk_refs[j][:, i * third : (i + 1) * third] = part
            if j:
                others_ref[:, (3 * j - 3 + i) * third : (3 * j - 2 + i) * third] = part
            ffn_ref[:, (3 * j + i) * third : (3 * j + i + 1) * third] = part


def pack(info, o, g, u, d):
    rows, units = g.shape
    feats = o.shape[0]
    widths = (feats, 3 * units, units, units, units, 2 * units)
    return pl.pallas_call(
        pack_kernel,
        in_specs=[SMEM] + [ANY] * 4,
        out_specs=[pl.BlockSpec(memory_space=pltpu.VMEM)] * 6,
        out_shape=[shape_of((rows, n), BF16) for n in widths],
        scratch_shapes=[pltpu.VMEM(a.shape, BF16) for a in (o, g, u, d)]
        + [pltpu.SemaphoreType.DMA((4,))],
        compiler_params=pltpu.CompilerParams(vmem_limit_bytes=24 << 20),
        cost_estimate=cost(False),
        name="pack",
    )(info, o, g, u, d)


def join_kernel(q_ref, k_ref, v_ref, out_ref):
    at = 0
    for ref in (q_ref, k_ref, v_ref):
        out_ref[:, at : at + ref.shape[1]] = ref[...]
        at += ref.shape[1]


def join(q, k, v):
    return pl.pallas_call(
        join_kernel,
        out_shape=shape_of((q.shape[0], q.shape[1] + k.shape[1] + v.shape[1]), BF16),
        compiler_params=pltpu.CompilerParams(vmem_limit_bytes=8 << 20),
        cost_estimate=cost(False),
        name="join",
    )(q, k, v)


def norm_one_kernel(info, tok_ref, gain_ref, x_ref, nt_ref, x32):
    quarter = x_ref.shape[1] // 4
    for p, mask in enumerate(MASKS):
        at = pl.multiple_of(jnp.bitwise_xor(info[1], mask) * quarter, quarter)
        part = tok_ref[0, :, pl.ds(at, quarter)]
        x_ref[:, p * quarter : (p + 1) * quarter] = part
        x32[:, p * quarter : (p + 1) * quarter] = part.astype(F32)
    x = x32[...]
    rho = lax.rsqrt(jnp.mean(x * x, axis=-1, keepdims=True) + EPS)
    nt_ref[...] = (x * rho * gain_ref[...]).T.astype(BF16)


def norm_one(info, tokens, gain, tile):
    _, tok, width = tokens.shape
    return pl.pallas_call(
        norm_one_kernel,
        grid_spec=pltpu.PrefetchScalarGridSpec(
            num_scalar_prefetch=1,
            grid=(tok // tile,),
            in_specs=[
                pl.BlockSpec((1, tile, width), lambda i, info: (info[0], i, 0)),
                pl.BlockSpec((1, width), lambda i, info: (0, 0)),
            ],
            out_specs=[
                pl.BlockSpec((tile, width), lambda i, info: (i, 0)),
                pl.BlockSpec((width, tile), lambda i, info: (0, i)),
            ],
            scratch_shapes=[pltpu.VMEM((tile, width), F32)],
        ),
        out_shape=[shape_of((tok, width), BF16), shape_of((width, tok), BF16)],
        compiler_params=settings(1, 24),
        cost_estimate=cost(False),
        name="norm_one",
    )(info, tokens, gain)


def proj_kernel(heads, block, plan, count, info, *refs):
    nt_ref, cos_ref, sin_ref, qg_ref, kg_ref, rot_ref, raw_ref, w_ref, sem = refs[count:]
    rows = w_ref.shape[0] // 4

    @pl.when(pl.program_id(0) == 0)
    def _():
        for k in range(4):

            @pl.when(block(info) == k)
            def _():
                for p, (piece, row) in enumerate(plan[k]):
                    src = refs[piece].at[pl.ds(row, rows)]
                    pltpu.make_async_copy(src, w_ref.at[pl.ds(p * rows, rows)], sem).start()

        pltpu.make_async_copy(w_ref, w_ref, sem).wait()

    hd = qg_ref.shape[0]
    half = hd // 2
    raw = dot(w_ref[...], nt_ref[...], 0, 0)
    cos_part, sin_part = cos_ref[...], sin_ref[...]
    heads_q, heads_k = heads
    raw_ref[...] = raw.astype(BF16)
    for h in range(heads_q + heads_k):
        v = raw[h * hd : (h + 1) * hd]
        rho = lax.rsqrt(jnp.mean(v * v, axis=0, keepdims=True) + EPS)
        v = v * rho * (qg_ref[...] if h < heads_q else kg_ref[...])
        a, b = v[:half], v[half:]
        rot_ref[h * hd : h * hd + half, :] = (a * cos_part - b * sin_part).astype(BF16)
        rot_ref[h * hd + half : (h + 1) * hd, :] = (b * cos_part + a * sin_part).astype(BF16)
    at = (heads_q + heads_k) * hd
    rot_ref[at:, :] = raw[at:].astype(BF16)


def project(info, weights, normed_t, cos_part, sin_part, gain_q, gain_k, heads, block):
    plan, pieces = weights
    width, tok = normed_t.shape
    cols = pieces[0].shape[1]
    tile = min(512, tok)
    const = lambda a: pl.BlockSpec(a.shape, lambda i, info: (0, 0))
    tab = lambda a: pl.BlockSpec((a.shape[0], tile), lambda i, info: (0, i))
    return pl.pallas_call(
        functools.partial(proj_kernel, heads, block, plan, len(pieces)),
        grid_spec=pltpu.PrefetchScalarGridSpec(
            num_scalar_prefetch=1,
            grid=(tok // tile,),
            in_specs=[ANY] * len(pieces)
            + [tab(normed_t), tab(cos_part), tab(sin_part), const(gain_q), const(gain_k)],
            out_specs=[pl.BlockSpec((cols, tile), lambda i, info: (0, i))] * 2,
            scratch_shapes=[pltpu.VMEM((width, cols), BF16), pltpu.SemaphoreType.DMA],
        ),
        out_shape=[shape_of((cols, tok), BF16), shape_of((cols, tok), BF16)],
        compiler_params=settings(1, 24),
        cost_estimate=cost(False),
        name="project",
    )(info, *pieces, normed_t, cos_part, sin_part, gain_q, gain_k)


def head_back_kernel(
    heads, info, dm_ref, dt_ref, rm_ref, rt_ref, cos_ref, sin_ref, qg_ref, kg_ref, out_ref, gg_ref
):
    step, part = pl.program_id(0), pl.program_id(1)
    hd = qg_ref.shape[0]
    half = hd // 2
    heads_q, heads_k = heads
    cos_part, sin_part = cos_ref[...], sin_ref[...]
    tile = cos_part.shape[1]

    @pl.when((step == 0) & (part == 0))
    def _():
        gg_ref[...] = jnp.zeros_like(gg_ref)

    def work(d_ref, r_ref):
        gain_q = jnp.zeros((hd, 1), F32)
        gain_k = jnp.zeros((hd, 1), F32)
        done = []
        for h in range(heads_q + heads_k):
            is_q = h < heads_q
            g = d_ref[h * hd : (h + 1) * hd, :].astype(F32)
            raw = r_ref[h * hd : (h + 1) * hd, :].astype(F32)
            a, b = g[:half], g[half:]
            turned = jnp.concatenate(
                [a * cos_part + b * sin_part, b * cos_part - a * sin_part], axis=0
            )
            rho = lax.rsqrt(jnp.mean(raw * raw, axis=0, keepdims=True) + EPS)
            unit = raw * rho
            prod = turned * unit
            scaled = turned * (qg_ref[...] if is_q else kg_ref[...])
            mean = jnp.mean(scaled * unit, axis=0, keepdims=True)
            done.append(rho * (scaled - unit * mean))
            total = jnp.sum(prod, axis=1, keepdims=True)
            if is_q:
                gain_q = gain_q + total
            else:
                gain_k = gain_k + total
        done.append(d_ref[(heads_q + heads_k) * hd :, :].astype(F32))
        out_ref[0] = jnp.concatenate(done, axis=0).T.astype(BF16)
        lane = lax.broadcasted_iota(jnp.int32, gg_ref.shape, 1)
        gg_ref[...] += jnp.where(lane == 0, gain_q, jnp.where(lane == 1, gain_k, 0.0))

    @pl.when(step == 0)
    def _():
        work(dm_ref, rm_ref)

    @pl.when(step == 1)
    def _():
        work(dt_ref, rt_ref)


def head_back(info, grad_mine, grad_theirs, raw_mine, raw_theirs, cos_part, sin_part, gq, gk, heads):
    cols, tok = grad_mine.shape
    tile = min(512, tok)
    mine = pl.BlockSpec((cols, tile), lambda s, i, info: (0, jnp.where(s == 0, i, tok // tile - 1)))
    theirs = pl.BlockSpec((cols, tile), lambda s, i, info: (0, jnp.where(s == 0, 0, i)))
    tab = lambda a: pl.BlockSpec((a.shape[0], tile), lambda s, i, info: (0, i))
    const = lambda a: pl.BlockSpec(a.shape, lambda s, i, info: (0, 0))
    return pl.pallas_call(
        functools.partial(head_back_kernel, heads),
        grid_spec=pltpu.PrefetchScalarGridSpec(
            num_scalar_prefetch=1,
            grid=(2, tok // tile),
            in_specs=[
                mine,
                theirs,
                mine,
                theirs,
                tab(cos_part),
                tab(sin_part),
                const(gq),
                const(gk),
            ],
            out_specs=[
                pl.BlockSpec(
                    (1, tile, cols), lambda s, i, info: (jnp.bitwise_xor(info[2], s), i, 0)
                ),
                pl.BlockSpec((gq.shape[0], 128), lambda s, i, info: (0, 0)),
            ],
        ),
        out_shape=[shape_of((2, tok, cols), BF16), shape_of((gq.shape[0], 128), F32)],
        compiler_params=settings(2, 60),
        cost_estimate=cost(False),
        name="head_back",
    )(info, grad_mine, grad_theirs, raw_mine, raw_theirs, cos_part, sin_part, gq, gk)


def load_rows(info, mine_ref, got_ref, rows, sems):
    tok = mine_ref.shape[1]
    ctx = info[2]
    here = pl.multiple_of(ctx * tok, tok)
    there = pl.multiple_of((1 - ctx) * tok, tok)
    one = pltpu.make_async_copy(mine_ref, rows.at[:, pl.ds(here, tok)], sems.at[0])
    two = pltpu.make_async_copy(got_ref, rows.at[:, pl.ds(there, tok)], sems.at[1])
    one.start()
    two.start()
    one.wait()
    two.wait()


def keys_with_bias(keys, length):
    hd, slots = keys.shape
    pos = lax.broadcasted_iota(jnp.int32, (hd, slots), 1)
    row = lax.broadcasted_iota(jnp.int32, (hd, slots), 0)
    bias = jnp.where((row == 0) & (pos >= length), NEGATIVE, 0.0)
    return jnp.concatenate([keys.astype(F32), bias], axis=0).T.astype(BF16)


def query_with_one(pair):
    one_row = jnp.where(lax.broadcasted_iota(jnp.int32, pair.shape, 0) == 0, 1.0, 0.0)
    return jnp.concatenate([pair, one_row.astype(BF16)], axis=0)


def by_halves(left, right):
    half = left.shape[1] // 2
    return jnp.concatenate(
        [left[:, :half], right[:, :half], left[:, half:], right[:, half:]], axis=1
    )


def by_heads(both):
    quarter = both.shape[1] // 4
    part = lambda i: both[:, i * quarter : (i + 1) * quarter]
    return (
        jnp.concatenate([part(0), part(2)], axis=1),
        jnp.concatenate([part(1), part(3)], axis=1),
    )


def causal(scores):
    half = scores.shape[0]
    key_pos = lax.broadcasted_iota(jnp.int32, (half, half), 0)
    query_pos = lax.broadcasted_iota(jnp.int32, (half, half), 1)
    allowed = key_pos <= query_pos
    return jnp.where(jnp.concatenate([allowed, allowed], axis=1), scores, NEGATIVE)


def attn_fwd_kernel(
    width, hd, info, mine_ref, got_ref, keep_ref, send_ref, lse_ref, rows, key_rows, sems
):
    head, block = pl.program_id(0), pl.program_id(1)
    heads_k = pl.num_programs(0)
    scale = hd**-0.5 * LOG2E
    length = info[3]
    key_at = pl.multiple_of(heads_k * 2 * hd + head * hd, hd)
    value_at = pl.multiple_of(heads_k * 3 * hd + head * hd, hd)
    query_at = pl.multiple_of(head * 2 * hd, 2 * hd)

    @pl.when((head == 0) & (block == 0))
    def _():
        load_rows(info, mine_ref, got_ref, rows, sems)

    @pl.when(block == 0)
    def _():
        key_rows[...] = keys_with_bias(rows[pl.ds(key_at, hd), :], length)

    start = pl.multiple_of(block * width, width)
    both = rows[pl.ds(query_at, 2 * hd), pl.ds(start, width)]
    query = query_with_one(by_halves(both[:hd], both[hd:]))

    def tile(at, carried, diagonal):
        out, total = carried
        scores = dot(key_rows[pl.ds(at, width), :], query, 1, 0)
        if diagonal:
            key_pos = lax.broadcasted_iota(jnp.int32, (width, width), 0)
            query_pos = lax.broadcasted_iota(jnp.int32, (width, width), 1)
            allowed = key_pos <= query_pos
            allowed = by_halves(allowed, allowed)
            scores = jnp.where(allowed, scores, NEGATIVE)
        probs = jnp.exp2(scores * scale)
        total = total + jnp.sum(probs, axis=0, keepdims=True)
        out = out + dot(rows[pl.ds(value_at, hd), pl.ds(at, width)], probs.astype(BF16), 1, 0)
        return out, total

    carried = (jnp.zeros((hd, 2 * width), F32), jnp.zeros((1, 2 * width), F32))
    full = jnp.minimum(block, lax.div(length + width - 1, width))
    carried = lax.fori_loop(
        0, full, lambda j, c: tile(pl.multiple_of(j * width, width), c, False), carried
    )
    out, total = tile(start, carried, True)
    out = out * (1.0 / total)
    out = jnp.concatenate(by_heads(out), axis=0).T.astype(BF16)
    here = block // 2 == info[2]

    @pl.when(here)
    def _():
        keep_ref[...] = out

    @pl.when(jnp.logical_not(here))
    def _():
        send_ref[...] = out

    log_first, log_second = by_heads(jnp.log2(total))
    lse_ref[0, 0:1, :] = log_first
    lse_ref[0, 1:2, :] = log_second


def keep_block(i, info):
    return jnp.clip(i - 2 * info[2], 0, 1)


def send_block(i, info):
    return jnp.clip(i - 2 * (1 - info[2]), 0, 1)


def attn_fwd(info, mine, got, hd):
    cols, tok = mine.shape
    heads_k = cols // (4 * hd)
    width = tok // 2
    return pl.pallas_call(
        functools.partial(attn_fwd_kernel, width, hd),
        grid_spec=pltpu.PrefetchScalarGridSpec(
            num_scalar_prefetch=1,
            grid=(heads_k, 4),
            in_specs=[ANY, ANY],
            out_specs=[
                pl.BlockSpec((width, 2 * hd), lambda h, i, info: (keep_block(i, info), h)),
                pl.BlockSpec((width, 2 * hd), lambda h, i, info: (send_block(i, info), h)),
                pl.BlockSpec((1, 2, width), lambda h, i, info: (h, 0, i)),
            ],
            scratch_shapes=[
                pltpu.VMEM((cols, 2 * tok), BF16),
                pltpu.VMEM((2 * tok, 2 * hd), BF16),
                pltpu.SemaphoreType.DMA((2,)),
            ],
        ),
        out_shape=[
            shape_of((tok, heads_k * 2 * hd), BF16),
            shape_of((tok, heads_k * 2 * hd), BF16),
            shape_of((heads_k, 2, 2 * tok), F32),
        ],
        compiler_params=settings(2, 60),
        cost_estimate=cost(True),
        name="attn_fwd",
    )(info, mine, got)


def attn_bwd_kernel(
    width,
    hd,
    info,
    mine_ref,
    got_ref,
    ok_ref,
    os_ref,
    gk_ref,
    gs_ref,
    lse_ref,
    keep_ref,
    send_ref,
    rows,
    key_rows,
    value_rows,
    key_sum,
    value_sum,
    sems,
):
    head, block = pl.program_id(0), pl.program_id(1)
    heads_k = pl.num_programs(0)
    scale = hd**-0.5
    length = info[3]
    ctx = info[2]
    tok = keep_ref.shape[1]
    key_at = pl.multiple_of(heads_k * 2 * hd + head * hd, hd)
    value_at = pl.multiple_of(heads_k * 3 * hd + head * hd, hd)
    query_at = pl.multiple_of(head * 2 * hd, 2 * hd)

    @pl.when((head == 0) & (block == 0))
    def _():
        load_rows(info, mine_ref, got_ref, rows, sems)

    @pl.when(block == 0)
    def _():
        key_rows[...] = keys_with_bias(rows[pl.ds(key_at, hd), :], length)
        value_rows[...] = rows[pl.ds(value_at, hd), :].astype(F32).T.astype(BF16)
        key_sum[...] = jnp.zeros_like(key_sum)
        value_sum[...] = jnp.zeros_like(value_sum)

    start = pl.multiple_of(block * width, width)
    here = block // 2 == ctx

    def store_query(value):
        at = pl.ds(pl.multiple_of((block % 2) * width, width), width)

        @pl.when(here)
        def _():
            keep_ref[pl.ds(query_at, 2 * hd), at] = value

        @pl.when(jnp.logical_not(here))
        def _():
            send_ref[pl.ds(query_at, 2 * hd), at] = value

    @pl.when(block * width < length)
    def _():
        both = rows[pl.ds(query_at, 2 * hd), pl.ds(start, width)]
        pair = by_halves(both[:hd], both[hd:])
        query = query_with_one(pair)
        query_rows = pair.astype(F32).T.astype(BF16)
        grad_wide = jnp.where(here, gk_ref[...].astype(F32), gs_ref[...].astype(F32))
        out_wide = jnp.where(here, ok_ref[...].astype(F32), os_ref[...].astype(F32))
        grad_t = grad_wide.T
        prod = (grad_wide * out_wide).T
        grad = by_halves(grad_t[:hd], grad_t[hd:]).astype(BF16)
        half = width // 2
        grad_rows = jnp.concatenate(
            [
                grad_wide[:half, :hd],
                grad_wide[:half, hd:],
                grad_wide[half:, :hd],
                grad_wide[half:, hd:],
            ],
            axis=0,
        ).astype(BF16)
        delta = by_halves(
            jnp.sum(prod[:hd], axis=0, keepdims=True), jnp.sum(prod[hd:], axis=0, keepdims=True)
        )
        lse = by_halves(lse_ref[0, 0:1, :], lse_ref[0, 1:2, :])

        def terms(at, keys, first, mask):
            scores = dot(key_rows[pl.ds(at, keys), :], query[:, first:], 1, 0)
            if mask:
                part = causal(scores[:, :width])
                wide = scores.shape[1] > width
                scores = jnp.concatenate([part, scores[:, width:]], axis=1) if wide else part
            probs = jnp.exp2(scores * (scale * LOG2E) - lse[:, first:])
            grad_probs = dot(value_rows[pl.ds(at, keys), :], grad[:, first:], 1, 0)
            grad_scores = (probs * (grad_probs - delta[:, first:])).astype(BF16)
            value_sum[pl.ds(at, keys), :] += dot(probs.astype(BF16), grad_rows[first:], 1, 0)
            key_sum[pl.ds(at, keys), :] += dot(grad_scores, query_rows[first:], 1, 0)
            return dot(rows[pl.ds(key_at, hd), pl.ds(at, keys)], grad_scores, 1, 0)

        query_sum = lax.fori_loop(
            0,
            block,
            lambda j, s: s + terms(pl.multiple_of(j * width, width), width, 0, False),
            jnp.zeros((hd, 2 * width), F32),
        )
        query_sum = query_sum + terms(start, half, 0, True)
        later = terms(pl.multiple_of(start + half, half), half, width, True)
        query_sum = jnp.concatenate([query_sum[:, :width], query_sum[:, width:] + later], axis=1)
        store_query(jnp.concatenate(by_heads(query_sum * scale), axis=0).astype(BF16))

    @pl.when(block * width >= length)
    def _():
        store_query(jnp.zeros((2 * hd, width), BF16))

    @pl.when(block == 3)
    def _():
        for at, total in ((key_at, key_sum[...] * scale), (value_at, value_sum[...])):
            total = total.T.astype(BF16)
            left, right = total[:, :tok], total[:, tok:]

            @pl.when(ctx == 0)
            def _():
                keep_ref[pl.ds(at, hd), :] = left
                send_ref[pl.ds(at, hd), :] = right

            @pl.when(ctx == 1)
            def _():
                keep_ref[pl.ds(at, hd), :] = right
                send_ref[pl.ds(at, hd), :] = left


def attn_bwd(info, mine, got, out_keep, out_send, grad_keep, grad_send, lse, hd):
    cols, tok = mine.shape
    heads_k = cols // (4 * hd)
    width = tok // 2
    keep = pl.BlockSpec((width, 2 * hd), lambda h, i, info: (keep_block(i, info), h))
    send = pl.BlockSpec((width, 2 * hd), lambda h, i, info: (send_block(i, info), h))
    full = pl.BlockSpec((cols, tok), lambda h, i, info: (0, 0))
    return pl.pallas_call(
        functools.partial(attn_bwd_kernel, width, hd),
        grid_spec=pltpu.PrefetchScalarGridSpec(
            num_scalar_prefetch=1,
            grid=(heads_k, 4),
            in_specs=[
                ANY,
                ANY,
                keep,
                send,
                keep,
                send,
                pl.BlockSpec((1, 2, width), lambda h, i, info: (h, 0, i)),
            ],
            out_specs=[full, full],
            scratch_shapes=[
                pltpu.VMEM((cols, 2 * tok), BF16),
                pltpu.VMEM((2 * tok, 2 * hd), BF16),
                pltpu.VMEM((2 * tok, hd), BF16),
                pltpu.VMEM((2 * tok, hd), F32),
                pltpu.VMEM((2 * tok, hd), F32),
                pltpu.SemaphoreType.DMA((2,)),
            ],
        ),
        out_shape=[shape_of((cols, tok), BF16), shape_of((cols, tok), BF16)],
        compiler_params=settings(2, 60),
        cost_estimate=cost(True, 16.2),
        name="attn_bwd",
    )(info, mine, got, out_keep, out_send, grad_keep, grad_send, lse)


def load_blocks(plan, pieces, target, sem):
    rows = target.shape[1] // 4

    @pl.when(pl.program_id(0) == 0)
    def _():
        for k, places in enumerate(plan):
            for p, (piece, row) in enumerate(places):
                src = pieces[piece].at[pl.ds(row, rows)]
                pltpu.make_async_copy(src, target.at[k, pl.ds(p * rows, rows)], sem).start()
        pltpu.make_async_copy(target, target, sem).wait()


def out_proj_kernel(plan, count, info, *refs):
    x_ref, a0, a1, b0, b1, gain_ref, r_ref, n_ref, nt_ref, att_ref, w_ref, sem = refs[count:]
    load_blocks(plan, refs, w_ref, sem)
    ctx = info[2]
    total = x_ref[...].astype(F32)
    for j, ref, side in ((0, a0, ctx), (1, a1, ctx), (0, b0, 1 - ctx), (1, b1, 1 - ctx)):
        block = 2 * side + j
        part = ref[...]
        att_ref[block] = part
        total = total + dot(part, w_ref[block], 1, 1)
    rho = lax.rsqrt(jnp.mean(total * total, axis=-1, keepdims=True) + EPS)
    normed = total * rho * gain_ref[...]
    r_ref[...] = total
    n_ref[...] = normed.astype(BF16)
    nt_ref[...] = normed.T.astype(BF16)


def out_proj(info, x, mine, theirs, weights, gain, tile):
    plan, pieces = weights
    tok, width = x.shape
    feats = pieces[0].shape[1]
    rows_of = lambda n: pl.BlockSpec((tile, n), lambda i, info: (i, 0))
    return pl.pallas_call(
        functools.partial(out_proj_kernel, plan, len(pieces)),
        grid_spec=pltpu.PrefetchScalarGridSpec(
            num_scalar_prefetch=1,
            grid=(tok // tile,),
            in_specs=[ANY] * len(pieces)
            + [rows_of(width)]
            + [rows_of(feats)] * 4
            + [pl.BlockSpec((1, width), lambda i, info: (0, 0))],
            out_specs=[
                rows_of(width),
                rows_of(width),
                pl.BlockSpec((width, tile), lambda i, info: (0, i)),
                pl.BlockSpec((4, tile, feats), lambda i, info: (0, i, 0)),
            ],
            scratch_shapes=[pltpu.VMEM((4, width, feats), BF16), pltpu.SemaphoreType.DMA],
        ),
        out_shape=[
            shape_of((tok, width), F32),
            shape_of((tok, width), BF16),
            shape_of((width, tok), BF16),
            shape_of((4, tok, feats), BF16),
        ],
        compiler_params=settings(1, 60),
        cost_estimate=cost(True),
        name="out_proj",
    )(info, *pieces, x, *mine, *theirs, gain)


def norm_two_back_kernel(plan, count, info, *refs):
    g_ref, r_ref, gr_ref, gain_ref, gres_ref, gat_ref, a0, a1, b0, b1, gg_ref, w_ref, sem = refs[count:]
    load_blocks(plan, refs, w_ref, sem)
    ctx = info[2]
    grad, resid = g_ref[...], r_ref[...]
    rho = lax.rsqrt(jnp.mean(resid * resid, axis=-1, keepdims=True) + EPS)
    unit = resid * rho
    scaled = grad * gain_ref[...]
    back = rho * (scaled - unit * jnp.mean(scaled * unit, axis=-1, keepdims=True))
    total = gr_ref[...] + back
    gres_ref[...] = total
    low = total.astype(BF16)
    gat_ref[...] = total.T.astype(BF16)

    @pl.when(pl.program_id(0) == 0)
    def _():
        gg_ref[...] = jnp.zeros_like(gg_ref)

    gg_ref[...] += jnp.sum(grad * unit, axis=0, keepdims=True)
    for j, ref, side in ((0, a0, ctx), (1, a1, ctx), (0, b0, 1 - ctx), (1, b1, 1 - ctx)):
        ref[...] = dot(low, w_ref[2 * side + j], 1, 0).astype(BF16)


def norm_two_back(info, grad, resid, grad_result, gain, weights, tile):
    plan, pieces = weights
    tok, width = grad.shape
    feats = pieces[0].shape[1]
    rows_of = lambda n: pl.BlockSpec((tile, n), lambda i, info: (i, 0))
    row = pl.BlockSpec((1, width), lambda i, info: (0, 0))
    return pl.pallas_call(
        functools.partial(norm_two_back_kernel, plan, len(pieces)),
        grid_spec=pltpu.PrefetchScalarGridSpec(
            num_scalar_prefetch=1,
            grid=(tok // tile,),
            in_specs=[ANY] * len(pieces) + [rows_of(width)] * 3 + [row],
            out_specs=[rows_of(width), pl.BlockSpec((width, tile), lambda i, info: (0, i))]
            + [rows_of(feats)] * 4
            + [row],
            scratch_shapes=[pltpu.VMEM((4, width, feats), BF16), pltpu.SemaphoreType.DMA],
        ),
        out_shape=[shape_of((tok, width), F32), shape_of((width, tok), BF16)]
        + [shape_of((tok, feats), BF16)] * 4
        + [shape_of((1, width), F32)],
        compiler_params=settings(1, 60),
        cost_estimate=cost(True, 5.4),
        name="norm_two_back",
    )(info, *pieces, grad, resid, grad_result, gain)


def norm_one_back_kernel(plan, count, info, *refs):
    p0, p1, x_ref, gres_ref, gain_ref, out_ref, gg_ref, w_ref, sem = refs[count:]
    load_blocks(plan, refs, w_ref, sem)
    quarter = x_ref.shape[1] // 4
    grad = dot(p0[0], w_ref[0], 1, 1)
    grad = grad + dot(p1[0], w_ref[1], 1, 1)
    grad = grad + dot(p0[1], w_ref[2], 1, 1)
    grad = grad + dot(p1[1], w_ref[3], 1, 1)
    x = x_ref[...].astype(F32)
    rho = lax.rsqrt(jnp.mean(x * x, axis=-1, keepdims=True) + EPS)
    unit = x * rho
    scaled = grad * gain_ref[...]
    back = rho * (scaled - unit * jnp.mean(scaled * unit, axis=-1, keepdims=True))
    total = (gres_ref[...] + back).astype(BF16)
    for p, mask in enumerate(MASKS):
        at = pl.multiple_of(jnp.bitwise_xor(info[1], mask) * quarter, quarter)
        part = total[:, p * quarter : (p + 1) * quarter]

        out_ref[:, pl.ds(at, quarter)] = part

    @pl.when(pl.program_id(0) == 0)
    def _():
        gg_ref[...] = jnp.zeros_like(gg_ref)

    gg_ref[...] += jnp.sum(grad * unit, axis=0, keepdims=True)


def norm_one_back(info, pairs, weights, x, grad_resid, gain, tile, part):
    plan, pieces = weights
    tok, width = x.shape
    cols = pieces[0].shape[1]
    steps = tok // tile // 2
    first = part * steps
    rows_of = lambda n: pl.BlockSpec((tile, n), lambda i, info: (first + i, 0))
    out_rows = pl.BlockSpec((tile, width), lambda i, info: (i, 0))
    pair = pl.BlockSpec((2, tile, cols), lambda i, info: (0, first + i, 0))
    row = pl.BlockSpec((1, width), lambda i, info: (0, 0))
    return pl.pallas_call(
        functools.partial(norm_one_back_kernel, plan, len(pieces)),
        grid_spec=pltpu.PrefetchScalarGridSpec(
            num_scalar_prefetch=1,
            grid=(steps,),
            in_specs=[ANY] * len(pieces) + [pair, pair, rows_of(width), rows_of(width), row],
            out_specs=[out_rows, row],
            scratch_shapes=[pltpu.VMEM((4, width, cols), BF16), pltpu.SemaphoreType.DMA],
        ),
        out_shape=[shape_of((tok // 2, width), BF16), shape_of((1, width), F32)],
        compiler_params=settings(1, 60),
        cost_estimate=cost(True),
        name="norm_one_back",
    )(info, *pieces, *pairs, x, grad_resid, gain)


def weight_copies(plan, pieces, gate_up, down, gate_up_sem, down_sem):
    third = down.shape[1] // 3
    rows = down.shape[0] // 4
    wide, thin = [], []
    for p, chunks in enumerate(plan):
        block = pl.ds(p * rows, rows)
        for j, (piece, row, at) in enumerate(chunks):
            src = pieces[piece].at[pl.ds(row, rows)]
            wide.append(
                pltpu.make_async_copy(
                    src.at[:, pl.ds(at, 2 * third)],
                    gate_up.at[block, pl.ds(j * 2 * third, 2 * third)],
                    gate_up_sem,
                )
            )
            thin.append(
                pltpu.make_async_copy(
                    src.at[:, pl.ds(at + 2 * third, third)],
                    down.at[block, pl.ds(j * third, third)],
                    down_sem,
                )
            )
    return wide, thin


def split_act(act):
    third = act.shape[1] // 6
    part = lambda j: act[:, j * third : (j + 1) * third]
    return [(part(0), part(1)), (part(2), part(3)), (part(4), part(5))]


def ffn_fwd_kernel(tile, plans, last, info, scale, x_ref, in_ref, *rest):
    if last:
        teach_ref, rest = rest[0], rest[1:]
    pieces = []
    for plan in plans:
        count = 1 + max(place[0] for chunks in plan for place in chunks)
        pieces.append(rest[:count])
        rest = rest[count:]
    act_ref, hid_ref = rest[:2]
    if last:
        out_ref, gres_ref, low_ref, lowt_ref, sq_ref = rest[2:7]
        gate_up, down, total, sems = rest[7:]
    else:
        sum_ref, gate_up, down, total, sems = rest[2:]
    step, part = pl.program_id(0), pl.program_id(1)
    final = len(plans) - 1
    width = x_ref.shape[1]
    quarter = width // 4
    third = down.shape[2] // 3

    def copies(s):
        return weight_copies(
            plans[s], pieces[s], gate_up.at[s], down.at[s], sems.at[s, 0], sems.at[s, 1]
        )

    @pl.when((step == 0) & (part == 0))
    def _():
        for s in range(len(plans)):
            wide, thin = copies(s)
            for copy in wide + thin:
                copy.start()

    for s in range(len(plans)):

        @pl.when((step == s) & (part == 0))
        def _():
            pltpu.make_async_copy(gate_up.at[s], gate_up.at[s], sems.at[s, 0]).wait()

    rows = pl.ds(pl.multiple_of(part * tile, tile), tile)
    act = dot(x_ref[rows, :], gate_up[step], 1, 0)
    for j, (gate, upper) in enumerate(split_act(act)):
        sig = sigmoid(gate)
        silu = gate * sig
        hid_ref[0, :, j * third : (j + 1) * third] = (silu * upper).astype(BF16)
        at = 2 * j * third
        act_ref[0, :, at : at + third] = (upper * (sig + silu - silu * sig)).astype(BF16)
        act_ref[0, :, at + third : at + 2 * third] = silu.astype(BF16)
    for s in range(len(plans)):

        @pl.when((step == s) & (part == 0))
        def _():
            pltpu.make_async_copy(down.at[s], down.at[s], sems.at[s, 1]).wait()

    grown = dot(hid_ref[0], down[step], 1, 1)

    @pl.when(step == 0)
    def _():
        total[rows, :] = in_ref[...] + grown

    @pl.when(step > 0)
    def _():
        total[rows, :] += grown

    @pl.when(step == final)
    def _():
        result = total[rows, :]
        if not last:
            sum_ref[...] = result
            return
        tok = x_ref.shape[0]
        slot = info[2] * tok + part * tile + lax.broadcasted_iota(jnp.int32, (tile, 1), 0)
        valid = jnp.where(slot < info[3], 1.0, 0.0)
        square = jnp.zeros((tile, quarter), F32)
        for p, mask in enumerate(MASKS):
            at = pl.multiple_of(jnp.bitwise_xor(info[1], mask) * quarter, quarter)
            cols = slice(p * quarter, (p + 1) * quarter)
            value = result[:, cols]
            out_ref[:, pl.ds(at, quarter)] = value.astype(BF16)
            error = valid * (value - teach_ref[0, :, pl.ds(at, quarter)].astype(F32))
            square = square + error * error
            grad = error * scale[0]
            gres_ref[:, cols] = grad
            low_ref[:, cols] = grad.astype(BF16)
            lowt_ref[cols, :] = grad.T.astype(BF16)

        @pl.when(part == 0)
        def _():
            sq_ref[...] = jnp.zeros_like(sq_ref)

        sq_ref[...] += jnp.sum(square, axis=0, keepdims=True)


def ffn_fwd(info, scale, x, total, teacher, weights, units, tile):
    tok, width = x.shape
    pieces = [piece for _, group in weights for piece in group]
    count = len(weights)
    last = teacher is not None
    entry = lambda s, i: jnp.where(s == 0, i, tok // tile - 1)
    leave = lambda s, i: jnp.where(s == count - 1, i, 0)
    tiles = lambda n: pl.BlockSpec((tile, n), lambda s, i, info: (leave(s, i), 0))
    slab = lambda n: pl.BlockSpec((1, tile, n), lambda s, i, info: (s, i, 0))
    in_specs = [
        SMEM,
        whole((tok, width)),
        pl.BlockSpec((tile, width), lambda s, i, info: (entry(s, i), 0)),
    ]
    out_specs = [slab(2 * units), slab(units)]
    out_shape = [shape_of((count, tok, 2 * units), BF16), shape_of((count, tok, units), BF16)]
    if last:
        in_specs.append(
            pl.BlockSpec((1, tile, width), lambda s, i, info: (info[0], leave(s, i), 0))
        )
        out_specs += [
            tiles(width),
            tiles(width),
            tiles(width),
            pl.BlockSpec((width, tile), lambda s, i, info: (0, leave(s, i))),
            pl.BlockSpec((1, width // 4), lambda s, i, info: (0, 0)),
        ]
        out_shape += [
            shape_of((tok, width), BF16),
            shape_of((tok, width), F32),
            shape_of((tok, width), BF16),
            shape_of((width, tok), BF16),
            shape_of((1, width // 4), F32),
        ]
    else:
        out_specs.append(tiles(width))
        out_shape.append(shape_of((tok, width), F32))
    return pl.pallas_call(
        functools.partial(ffn_fwd_kernel, tile, [plan for plan, _ in weights], last),
        grid_spec=pltpu.PrefetchScalarGridSpec(
            num_scalar_prefetch=1,
            grid=(count, tok // tile),
            in_specs=in_specs + [ANY] * len(pieces),
            out_specs=out_specs,
            scratch_shapes=[
                pltpu.VMEM((count, width, 2 * units), BF16),
                pltpu.VMEM((count, width, units), BF16),
                pltpu.VMEM((tok, width), F32),
                pltpu.SemaphoreType.DMA((count, 2)),
            ],
        ),
        out_shape=out_shape,
        compiler_params=settings(2, 60),
        cost_estimate=cost(True),
        name="ffn_fwd",
    )(info, scale, x, total, *([teacher] if last else []), *pieces)


def ffn_bwd_kernel(steps, plan, first, low_ref, act_ref, hid_ref, xt_ref, lowt_ref, *rest):
    count = 1 + max(place[0] for chunks in plan for place in chunks)
    pieces, rest = rest[:count], rest[count:]
    if not first:
        in_ref, rest = rest[0], rest[1:]
    out_ref, keep_ref, send_ref, gate_up, down, dact_all, hid_all, sems = rest
    step = pl.program_id(0)
    units = down.shape[1]
    third = units // 3
    tile = low_ref.shape[0]

    @pl.when(step == 0)
    def _():
        wide, thin = weight_copies(plan, pieces, gate_up, down, sems.at[0], sems.at[1])
        for copy in thin + wide:
            copy.start()
        pltpu.make_async_copy(down, down, sems.at[1]).wait()

    @pl.when(step < steps)
    def _():
        rows = pl.ds(pl.multiple_of(step * tile, tile), tile)
        grad_hidden = dot(low_ref[...], down[...], 1, 0)
        for j, (to_gate, to_upper) in enumerate(split_act(act_ref[0])):
            grad = grad_hidden[:, j * third : (j + 1) * third]
            at = 2 * j * third
            dact_all[rows, at : at + third] = (grad * to_gate.astype(F32)).astype(BF16)
            dact_all[rows, at + third : at + 2 * third] = (grad * to_upper.astype(F32)).astype(BF16)
        hid_all[rows, :] = hid_ref[0]

        @pl.when(step == 0)
        def _():
            pltpu.make_async_copy(gate_up, gate_up, sems.at[0]).wait()

        grown = dot(dact_all[rows, :], gate_up[...], 1, 1)
        out_ref[...] = grown if first else in_ref[...] + grown

    def weight_rows(target):
        target[:, : 2 * units] = dot(xt_ref[...], dact_all[...], 1, 0).astype(BF16)
        target[:, 2 * units :] = dot(lowt_ref[...], hid_all[...], 1, 0).astype(BF16)

    @pl.when((step >= steps) & (step < steps + 2))
    def _():
        weight_rows(send_ref)

    @pl.when(step >= steps + 2)
    def _():
        weight_rows(keep_ref)


def ffn_bwd(low, saved, weights, total, xt, lowt, tile):
    plan, pieces = weights
    acts, hiddens, block = saved
    tok, width = low.shape
    units = hiddens.shape[2]
    steps = tok // tile
    quarter = width // 4
    first = total is None
    clip = lambda i: jnp.minimum(i, steps - 1)
    rows_of = lambda n: pl.BlockSpec((tile, n), lambda i: (clip(i), 0))
    slab = lambda n: pl.BlockSpec((1, tile, n), lambda i: (block, clip(i), 0))
    feature = lambda i: (jnp.where(i < steps + 2, jnp.maximum(i - steps, 0) + 2, i - steps - 2), 0)
    return pl.pallas_call(
        functools.partial(ffn_bwd_kernel, steps, plan, first),
        grid=(steps + 4,),
        in_specs=[
            rows_of(width),
            slab(2 * units),
            slab(units),
            pl.BlockSpec((quarter, tok), feature),
            pl.BlockSpec((quarter, tok), feature),
        ]
        + [ANY] * len(pieces)
        + ([] if first else [rows_of(width)]),
        out_specs=[
            rows_of(width),
            pl.BlockSpec((quarter, 3 * units), lambda i: (jnp.maximum(i - steps - 2, 0), 0)),
            pl.BlockSpec((quarter, 3 * units), lambda i: (jnp.clip(i - steps, 0, 1), 0)),
        ],
        out_shape=[
            shape_of((tok, width), F32),
            shape_of((width // 2, 3 * units), BF16),
            shape_of((width // 2, 3 * units), BF16),
        ],
        scratch_shapes=[
            pltpu.VMEM((width, 2 * units), BF16),
            pltpu.VMEM((width, units), BF16),
            pltpu.VMEM((tok, 2 * units), BF16),
            pltpu.VMEM((tok, units), BF16),
            pltpu.SemaphoreType.DMA((2,)),
        ],
        input_output_aliases={} if first else {5 + len(pieces): 0},
        compiler_params=settings(1, 60),
        cost_estimate=cost(True, 11.2),
        name="ffn_bwd",
    )(low, acts, hiddens, xt, lowt, *pieces, *([] if first else [total]))


def turn_chunks(block):
    wide = block.shape[1] * 2 // 9
    thin = wide // 2
    starts = [(2 * wide, wide), (wide, wide), (0, wide)]
    starts += [(3 * wide + 2 * thin, thin), (3 * wide + thin, thin), (3 * wide, thin)]
    return jnp.concatenate([block[:, a : a + n] for a, n in starts], axis=1)


def sum_kernel(turns, *refs):
    total = None
    for ref, turn in zip(refs[:-1], turns):
        value = ref[...].astype(F32)
        value = turn_chunks(value) if turn else value
        total = value if total is None else total + value
    refs[-1][...] = total.astype(refs[-1].dtype)


def summed(terms, turns=None, dtype=BF16):
    rows, cols = terms[0].shape
    spec = pl.BlockSpec((128, cols), lambda i: (i, 0))
    return pl.pallas_call(
        functools.partial(sum_kernel, turns or [False] * len(terms)),
        grid=(rows // 128,),
        in_specs=[spec] * len(terms),
        out_specs=spec,
        out_shape=shape_of((rows, cols), dtype),
        compiler_params=settings(1, 60),
        cost_estimate=cost(False),
        name="summed",
    )(*terms)


def sums_kernel(jobs, count, info, *refs):
    arrays, refs = refs[:count], refs[count:]
    outs, (term_buf, out_buf, term_sems, out_sems) = refs[: len(jobs)], refs[len(jobs) :]
    rows = term_buf.shape[1]
    copies = []
    for terms in jobs:
        group = []
        for array, base, pick, _ in terms:
            at = base
            if pick is not None:
                at = pl.multiple_of(base + jnp.bitwise_xor(info[2], pick) * rows, rows)
            i = len(copies) + len(group)
            src = arrays[array].at[pl.ds(at, rows)]
            group.append(pltpu.make_async_copy(src, term_buf.at[i], term_sems.at[i]))
            group[-1].start()
        copies += group
    first = 0
    stores = []
    for j, terms in enumerate(jobs):
        total = None
        for i, (_, _, _, turn) in enumerate(terms):
            copies[first + i].wait()
            value = term_buf[first + i].astype(F32)
            value = turn_chunks(value) if turn else value
            total = value if total is None else total + value
        first += len(terms)
        out_buf[j] = total.astype(BF16)
        stores.append(pltpu.make_async_copy(out_buf.at[j], outs[j], out_sems.at[j]))
        stores[-1].start()
    for store in stores:
        store.wait()


def sums(info, arrays, jobs):
    cols = arrays[0].shape[1]
    rows, terms = 128, sum(len(job) for job in jobs)
    return pl.pallas_call(
        functools.partial(sums_kernel, jobs, len(arrays)),
        grid_spec=pltpu.PrefetchScalarGridSpec(
            num_scalar_prefetch=1,
            grid=(1,),
            in_specs=[ANY] * len(arrays),
            out_specs=[ANY] * len(jobs),
            scratch_shapes=[
                pltpu.VMEM((terms, rows, cols), BF16),
                pltpu.VMEM((len(jobs), rows, cols), BF16),
                pltpu.SemaphoreType.DMA((terms,)),
                pltpu.SemaphoreType.DMA((len(jobs),)),
            ],
        ),
        out_shape=[shape_of((rows, cols), BF16)] * len(jobs),
        compiler_params=settings(1, 60),
        cost_estimate=cost(False),
        name="sums",
    )(info, *arrays)


def core_jobs(keep, came):
    return [[(a, far * 256, pick, False) for a in (keep, came)] for far in (0, 1) for pick in (0, 1)]


def core_sum_kernel(info, left_ref, right_ref, *outs):
    total = (left_ref[...].astype(F32) + right_ref[...].astype(F32)).astype(BF16)
    block = pl.program_id(1)
    place = block // 2 * 2 + jnp.bitwise_xor(block % 2, info[2])
    for i, out in enumerate(outs):

        @pl.when(place == i)
        def _():
            out[...] = total


def core_sum(info, keep, came):
    groups, rows, cols = keep.shape
    spec = pl.BlockSpec((1, rows // 4, cols), lambda g, i, info: (g, i, 0))
    return pl.pallas_call(
        core_sum_kernel,
        grid_spec=pltpu.PrefetchScalarGridSpec(
            num_scalar_prefetch=1,
            grid=(groups, 4),
            in_specs=[spec] * 2,
            out_specs=[pl.BlockSpec((1, rows // 4, cols), lambda g, i, info: (g, 0, 0))] * 4,
        ),
        out_shape=[shape_of((groups, rows // 4, cols), BF16)] * 4,
        compiler_params=settings(2, 24),
        cost_estimate=cost(False),
        name="core_sum",
    )(info, keep, came)


def weight_grad_kernel(nt_ref, back0_ref, back1_ref, gt_ref, att_ref, keep_ref, send_ref):
    cols = back0_ref.shape[2]
    part, block = pl.program_id(0), pl.program_id(1)

    def rows(target, back_ref):
        target[0, :, :cols] = dot(nt_ref[...], back_ref[0], 1, 0).astype(BF16)
        target[0, :, cols:] = dot(gt_ref[...], att_ref[0], 1, 0).astype(BF16)

    for j, back_ref in enumerate((back0_ref, back1_ref)):

        @pl.when((part == 0) & (block % 2 == j))
        def _():
            rows(send_ref, back_ref)

        @pl.when((part == 1) & (block % 2 == j))
        def _():
            rows(keep_ref, back_ref)


def weight_grad(normed_t, backs, grad_t, attended):
    width, tok = normed_t.shape
    cols, feats = backs[0].shape[2], attended.shape[2]
    half = pl.BlockSpec((width // 2, tok), lambda p, k: (1 - p, 0))
    side = pl.BlockSpec((1, tok, cols), lambda p, k: (k // 2, 0, 0))
    shape = (1, width // 2, cols + feats)
    return pl.pallas_call(
        weight_grad_kernel,
        grid=(2, 4),
        in_specs=[half, side, side, half, pl.BlockSpec((1, tok, feats), lambda p, k: (k, 0, 0))],
        out_specs=[
            pl.BlockSpec(shape, lambda p, k: (jnp.where(p == 0, 0, k), 0, 0)),
            pl.BlockSpec(shape, lambda p, k: (jnp.where(p == 0, k, 3), 0, 0)),
        ],
        out_shape=[shape_of((4, width // 2, cols + feats), BF16)] * 2,
        compiler_params=settings(2, 60),
        cost_estimate=cost(True),
        name="weight_grad",
    )(normed_t, *backs, grad_t, attended)


def after(value, *others):
    return lax.optimization_barrier((value,) + others)[0]


def per_device_rows(
    tokens,
    teacher,
    lengths,
    attn_gain,
    q_weight,
    k_weight,
    v_weight,
    q_gain,
    k_gain,
    o_weight,
    ffn_gain,
    gate_weight,
    up_weight,
    down_weight,
):
    z = lax.axis_index("tp")
    ctx = lax.axis_index("ctx")
    fsdp = lax.axis_index("fsdp")
    rows_dev, tok, width = tokens.shape
    quarter = width // 4
    hd = q_gain.shape[0] * 4
    q_cols, k_cols = q_weight.shape[1], k_weight.shape[1]
    proj = q_cols + 2 * k_cols
    heads = (q_cols // hd, k_cols // hd)
    units = gate_weight.shape[1]
    slots = rows_dev * 4 * tok * 2

    def x_swap(v):
        return lax.ppermute(v, "fsdp", X_SWAP)

    def core_swap(v):
        return lax.ppermute(v, "fsdp", CORE_SWAP)

    def y_swap(v):
        return lax.ppermute(v, "ctx", Y_SWAP)

    def z_up(v):
        return lax.ppermute(v, "tp", Z_UP)

    def z_far(v):
        return lax.ppermute(v, "tp", Z_FAR)

    def z_down(v):
        return lax.ppermute(v, "tp", Z_DOWN)

    def natural(v):
        v = jnp.concatenate([v[0:1], v[2:3], v[1:2], v[3:4]], axis=0)
        v = jnp.where(fsdp % 2 == 0, v, jnp.concatenate([v[1:2], v[0:1], v[3:4], v[2:3]], axis=0))
        return jnp.where(fsdp // 2 == 0, v, jnp.concatenate([v[2:4], v[0:2]], axis=0))

    v = {}

    def sync():
        v.update(lax.optimization_barrier(dict(v)))

    length = lax.dynamic_slice_in_dim(lengths, z, 1, 0)
    info = jnp.concatenate([jnp.stack([z, fsdp, ctx]).astype(jnp.int32), length])
    w_proj = join(q_weight, k_weight, v_weight)
    proj_z = [z_up(w_proj), z_far(w_proj), z_down(w_proj)]
    proj_own = jnp.concatenate([w_proj, x_swap(w_proj)], axis=0)
    count_here = jnp.sum(lengths).astype(F32)[None]
    vector = jnp.concatenate([attn_gain, ffn_gain, q_gain, k_gain]).astype(F32)
    vector = jnp.concatenate([vector, count_here, jnp.zeros((640 - 545,), F32)])[None]
    vector = jnp.concatenate([vector, x_swap(vector)], axis=0)
    vector = jnp.concatenate([vector, core_swap(vector)], axis=0)
    w_out, w_ffn, *w_chunks = pack(info, o_weight, gate_weight, up_weight, down_weight)
    pos = (ctx * tok + jnp.arange(tok, dtype=jnp.int32)).astype(F32)
    frequency = THETA ** (-(2.0 * jnp.arange(hd // 2, dtype=F32)) / hd)
    angles = frequency[:, None] * pos[None, :]
    head_gains = natural(vector[:, 2 * quarter : 544])
    v.update(
        info=info,
        proj_own=proj_own,
        proj_z=jnp.concatenate(proj_z, axis=0),
        w_out=w_out,
        w_ffn=w_ffn,
        w_chunks=w_chunks,
        gain_one=vector[:, :quarter].reshape(1, width),
        gain_two=vector[:, quarter : 2 * quarter].reshape(1, width),
        total_count=jnp.sum(vector[:, 544]),
        gain_q=head_gains[:, : hd // 4].reshape(hd, 1),
        gain_k=head_gains[:, hd // 4 :].reshape(hd, 1),
        cos_part=jnp.cos(angles),
        sin_part=jnp.sin(angles),
    )
    sync()
    info = v["info"]

    proj_zfar = x_swap(v["proj_z"])
    out_z = [z_up(v["w_out"]), z_far(v["w_out"]), z_down(v["w_out"])]
    own_core = core_swap(v["proj_own"])
    x_in, normed_one_t = norm_one(info, tokens, v["gain_one"], 256)
    v.update(
        proj_zfar=proj_zfar, own_core=own_core, x_in=x_in, normed_one_t=normed_one_t, out_z=out_z
    )
    sync()

    plan_proj = [[(0, 0), (0, quarter), (3, 0), (3, quarter)]]
    plan_proj += [[(p, k * quarter) for p in (1, 2, 4, 5)] for k in range(3)]
    weights_proj = [v["proj_own"], v["proj_z"], v["proj_zfar"], v["own_core"]]
    weights_proj += [core_swap(v["proj_z"]), core_swap(v["proj_zfar"])]
    one = [z_up(v["w_chunks"][0]), z_up(v["w_chunks"][3])]
    ffn_far = x_swap(v["w_ffn"])
    tables = [v[name] for name in ("cos_part", "sin_part", "gain_q", "gain_k")]

    def make(block, *then):
        normed_t = after(v["normed_one_t"], *then)
        return project(info, (plan_proj, weights_proj), normed_t, *tables, heads, block)

    theirs = [make(lambda s: 2 * (1 - s[2]))]
    got = [y_swap(theirs[0][0])]
    theirs.append(make(lambda s: 2 * (1 - s[2]) + 1, theirs[0][0]))
    got.append(y_swap(theirs[1][0]))
    mine = [make(lambda s: 2 * s[2], theirs[1][0])]
    mine.append(make(lambda s: 2 * s[2] + 1, mine[0][0]))
    v.update(
        one=one,
        ffn_far=ffn_far,
        weights_proj=weights_proj,
        mine=mine,
        theirs=theirs,
        got0=got[0],
    )
    sync()

    one_far = [x_swap(v["one"][0])]
    three = [z_down(v["w_chunks"][0])]
    own_cores = [core_swap(v["w_ffn"]), core_swap(v["ffn_far"])]
    first = attn_fwd(info, v["mine"][0][0], v["got0"], hd)
    v.update(first=first, got1=got[1], one_far=one_far, three=three, own_cores=own_cores)
    sync()

    arrived = [y_swap(v["first"][1])]
    three = v["three"] + [z_down(v["w_chunks"][1])]
    out_blocks = jnp.concatenate([v["w_out"]] + v["out_z"], axis=0)
    out_far = x_swap(out_blocks)
    one_cores = [core_swap(v["one"][0]), core_swap(v["one_far"][0])]
    second = attn_fwd(info, v["mine"][1][0], v["got1"], hd)
    v.update(
        second=second,
        arrived=arrived,
        three=three,
        out_blocks=out_blocks,
        out_far=out_far,
        one_cores=one_cores,
    )
    sync()

    arrived = v["arrived"] + [y_swap(v["second"][1])]
    three = v["three"] + [z_down(v["w_chunks"][2])]
    one_far = v["one_far"] + [x_swap(v["one"][1][:, :units])]
    weights_out = [v["out_blocks"], v["out_far"]]
    weights_out += [core_swap(v["out_blocks"]), core_swap(v["out_far"])]
    v.update(arrived=arrived, three=three, one_far=one_far, weights_out=weights_out)
    sync()

    plan_out = [[(p, k * quarter) for p in range(4)] for k in range(4)]
    two = [z_up(v["one"][0])]
    three_far = [x_swap(v["three"][0])]
    one_far = v["one_far"] + [y_swap(v["one_far"][0])]
    one_cores = v["one_cores"] + [core_swap(v["one"][1]), core_swap(v["one_far"][1])]
    resid, normed_two, normed_two_t, attended = out_proj(
        info,
        v["x_in"],
        [v["first"][0], v["second"][0]],
        v["arrived"],
        (plan_out, v["weights_out"]),
        v["gain_two"],
        256,
    )
    v.update(
        two=two,
        three_far=three_far,
        one_far=one_far,
        one_cores=one_cores,
        resid=resid,
        normed_two=normed_two,
        normed_two_t=normed_two_t,
        attended=attended,
    )
    sync()

    plan0 = [[(i, 0, j * units) for j in range(3)] for i in range(4)]
    plan_mixed = [[(0, 0, 0), (1, 0, 0), (1, 0, units)], [(i, 0, 0) for i in (2, 3, 4)]]
    plan_mixed += [[(5, 0, 0), (6, 0, 0), (6, 0, units)], [(i, 0, 0) for i in (7, 8, 9)]]
    scale = (slots / v["total_count"])[None]
    weights0 = [v["w_ffn"], v["ffn_far"]] + v["own_cores"]
    c0, cf, c1, cb = v["one_cores"]
    weights1 = v["one"] + v["one_far"] + [c0, c1, cf, cb, core_swap(v["one_far"][2])]
    two = v["two"] + [z_up(v["one"][1])]
    three_far = v["three_far"] + [x_swap(v["three"][1]), y_swap(v["three_far"][0])]
    two_far = [x_swap(v["two"][0])]
    three_cores = [core_swap(v["three"][0])]
    acts_a, hiddens_a, sum_a = ffn_fwd(
        info,
        scale,
        v["normed_two"],
        v["resid"],
        None,
        [(plan0, weights0), (plan_mixed, weights1)],
        units,
        256,
    )
    v.update(
        scale=scale,
        weights0=weights0,
        weights1=weights1,
        two=two,
        three_far=three_far,
        two_far=two_far,
        three_cores=three_cores,
        acts_a=acts_a,
        hiddens_a=hiddens_a,
        sum_a=sum_a,
    )
    sync()

    plan_chunks = [[(3 * p + j, 0, 0) for j in range(3)] for p in range(4)]
    weights3 = v["three"] + v["three_far"] + v["three_cores"]
    weights3 += [core_swap(part) for part in v["three"][1:]]
    weights3 += [core_swap(part) for part in v["three_far"]]
    two_far = v["two_far"] + [x_swap(v["two"][1][:, :units]), y_swap(v["two_far"][0])]
    two_cores = [core_swap(part) for part in v["two"] + v["two_far"]]
    acts_b, hiddens_b, sum_b = ffn_fwd(
        info, v["scale"], v["normed_two"], v["sum_a"], None, [(plan_chunks, weights3)], units, 256
    )
    v.update(
        weights3=weights3,
        two_far=two_far,
        two_cores=two_cores,
        acts_b=acts_b,
        hiddens_b=hiddens_b,
        sum_b=sum_b,
    )
    sync()

    weights2 = v["two"] + v["two_far"] + v["two_cores"]
    weights2 += [core_swap(part) for part in v["two_far"][1:]]
    acts_c, hiddens_c, result_low, grad_result, grad_low, grad_low_t, square = ffn_fwd(
        info, v["scale"], v["normed_two"], v["sum_b"], teacher, [(plan_mixed, weights2)], units, 256
    )
    v.update(
        weights2=weights2,
        acts_c=acts_c,
        hiddens_c=hiddens_c,
        result_low=result_low,
        grad_result=grad_result,
        grad_low=grad_low,
        grad_low_t=grad_low_t,
        square=square,
    )
    sync()

    def ffn_back(plan, weights, acts, hiddens, block, total):
        return ffn_bwd(
            v["grad_low"],
            (v[acts], v[hiddens], block),
            (plan, v[weights]),
            total,
            v["normed_two_t"],
            v["grad_low_t"],
            256,
        )

    turned = [False, False, True]
    output = lax.all_gather(v["result_low"], "tp", axis=0, tiled=False)
    total, keep2, send2 = ffn_back(plan_mixed, "weights2", "acts_c", "hiddens_c", 0, None)
    v.update(total=total, keep2=keep2, send2=send2)
    sync()

    came2 = core_swap(v["send2"])
    total, keep1, send1 = ffn_back(plan_mixed, "weights1", "acts_a", "hiddens_a", 1, v["total"])
    v.update(came2=came2, total=total, keep1=keep1, send1=send1)
    sync()

    came1 = core_swap(v["send1"])
    sum2 = sums(info, [v["keep2"], v["came2"]], core_jobs(0, 1))
    far_t2 = x_swap(sum2[3])
    total, keep3, send3 = ffn_back(
        plan_chunks, "weights3", "acts_b", "hiddens_b", 0, after(v["total"], sum2[0])
    )
    v.update(
        came1=came1,
        sum2=sum2,
        far_t2=far_t2,
        total=total,
        keep3=keep3,
        send3=send3,
    )
    sync()

    came3 = core_swap(v["send3"])
    far_h2 = x_swap(v["sum2"][2])
    there2, *sum1 = sums(
        info,
        [v["sum2"][1], v["far_t2"], v["keep1"], v["came1"]],
        [[(0, 0, None, False), (1, 0, None, False)]] + core_jobs(2, 3),
    )
    there2 = y_swap(there2)
    total, keep0, send0 = ffn_back(
        plan0, "weights0", "acts_a", "hiddens_a", 0, after(v["total"], sum1[0])
    )
    v.update(
        came3=came3,
        far_h2=far_h2,
        there2=there2,
        sum1=sum1,
        total=total,
        keep0=keep0,
        send0=send0,
    )
    sync()

    came0 = core_swap(v["send0"])
    far_t1 = x_swap(v["sum1"][3])
    plane = [(0, 0, None, False), (1, 0, None, False), (2, 0, None, True)]
    part2, *sum3 = sums(
        info,
        [v["sum2"][0], v["far_h2"], v["there2"], v["keep3"], v["came3"]],
        [plane] + core_jobs(3, 4),
    )
    down2 = z_down(part2)
    grad_resid, grad_attn_t, a0, a1, b0, b1, gain_two_sum = norm_two_back(
        info,
        after(v["total"], sum3[0]),
        v["resid"],
        v["grad_result"],
        v["gain_two"],
        (plan_out, v["weights_out"]),
        256,
    )
    grad_got = [y_swap(b0), y_swap(b1)]
    v.update(
        came0=came0,
        far_t1=far_t1,
        sum3=sum3,
        grad_resid=grad_resid,
        grad_attn_t=grad_attn_t,
        grad_mine=[a0, a1],
        gain_two_sum=gain_two_sum,
        grad_got0=grad_got[0],
    )
    sync()

    def attn_back(j, grad):
        out, got_ref = v["first" if j == 0 else "second"], v[f"got{j}"]
        return attn_bwd(
            info, v["mine"][j][0], got_ref, out[0], out[1], grad, v[f"grad_got{j}"], out[2], hd
        )

    far_h1 = x_swap(v["sum1"][2])
    there1, *sum0 = sums(
        info,
        [v["sum1"][1], v["far_t1"], v["keep0"], v["came0"]],
        [[(0, 0, None, False), (1, 0, None, False)]] + core_jobs(2, 3),
    )
    there1 = y_swap(there1)
    far_t3 = x_swap(v["sum3"][3])
    back0 = attn_back(0, after(v["grad_mine"][0], sum0[0]))
    v.update(
        far_h1=far_h1,
        there1=there1,
        far_t3=far_t3,
        down2=down2,
        sum0=sum0,
        back0=back0,
        grad_got1=grad_got[1],
    )
    sync()

    heads0 = y_swap(v["back0"][1])
    far_h3 = x_swap(v["sum3"][2])
    far_t0 = x_swap(v["sum0"][3])
    there3, two_down = sums(
        info,
        [v["sum3"][1], v["far_t3"], v["sum1"][0], v["far_h1"], v["there1"], v["down2"]],
        [
            [(0, 0, None, False), (1, 0, None, False)],
            [(2, 0, None, False), (3, 0, None, False), (4, 0, None, True), (5, 0, None, False)],
        ],
    )
    there3_got = y_swap(there3)
    two_down_got = z_down(two_down)
    back1 = attn_back(1, after(v["grad_mine"][1], there3, two_down, output))
    v.update(
        heads0=heads0, far_h3=far_h3, far_t0=far_t0, there3=there3_got, back1=back1
    )
    sync()

    heads1 = y_swap(v["back1"][1])
    far_h0 = x_swap(v["sum0"][2])
    part3, there0 = sums(
        info,
        [v["sum3"][0], v["far_h3"], v["there3"], v["sum0"][1], v["far_t0"]],
        [plane, [(3, 0, None, False), (4, 0, None, False)]],
    )
    up3 = z_up(part3)
    tables = [v[name] for name in ("cos_part", "sin_part", "gain_q", "gain_k")]
    head0 = head_back(
        info, v["back0"][0], v["heads0"], v["mine"][0][1], v["theirs"][0][1], *tables, heads
    )
    v.update(heads1=heads1, head0=head0, there0=there0)
    sync()

    there0 = y_swap(v["there0"])
    head1 = head_back(
        info, v["back1"][0], v["heads1"], v["mine"][1][1], v["theirs"][1][1], *tables, heads
    )
    def last_norm(part, *then):
        return norm_one_back(
            info,
            [v["head0"][0], after(head1[0], *then)],
            (plan_proj, v["weights_proj"]),
            v["x_in"],
            v["grad_resid"],
            v["gain_one"],
            tok // 4,
            part,
        )

    low_first, gain_first = last_norm(0)
    low_second, gain_second = last_norm(1, low_first)
    gathered = [lax.all_gather(low_first, "tp", axis=0, tiled=False)]
    tokens_low, gain_one_sum = low_second, gain_first + gain_second
    v.update(head1=head1, tokens_low=tokens_low, gain_one_sum=gain_one_sum, up3=up3)
    v.update(there0=there0, far_h0=far_h0, two_down=two_down_got)
    sync()

    gathered.append(lax.all_gather(v["tokens_low"], "tp", axis=0, tiled=False))
    keep, send = weight_grad(
        v["normed_one_t"], [v["head0"][0], v["head1"][0]], v["grad_attn_t"], v["attended"]
    )
    gain_heads = v["head0"][1] + v["head1"][1]
    vector = jnp.concatenate(
        [
            natural(v["gain_one_sum"].reshape(4, quarter)).reshape(1, width),
            natural(v["gain_two_sum"].reshape(4, quarter)).reshape(1, width),
            gain_heads[:, 0].reshape(1, hd),
            gain_heads[:, 1].reshape(1, hd),
            jnp.sum(v["square"]).reshape(1, 1),
            jnp.zeros((1, 127), F32),
        ],
        axis=1,
    )
    vector = vector + core_swap(vector)
    v.update(keep=keep, send=send)
    v.update(vector=vector)
    sync()

    rows = quarter // 2
    flat = lambda a: a.reshape(4 * rows, a.shape[-1])
    attn_sums = [flat(p) for p in core_sum(info, v["keep"], core_swap(v["send"]))]
    vector = v["vector"] + x_swap(v["vector"])
    v.update(sums=attn_sums, vector=vector)
    sync()

    far_t = x_swap(v["sums"][3])
    part0 = summed([v["sum0"][0], v["far_h0"], v["there0"]], turned)
    ffn_sum = summed([part0, v["two_down"], v["up3"]], None, F32)
    vector = v["vector"] + y_swap(v["vector"])
    v.update(far_t=far_t, ffn_sum=ffn_sum, vector=vector)
    sync()

    far_h = x_swap(v["sums"][2])
    there = y_swap(summed([v["sums"][1], v["far_t"]]))
    spread = jnp.zeros((rows_dev, tok, width), BF16)
    for j in range(2):
        part = output[:, j * tok // 2 : (j + 1) * tok // 2]
        spread = lax.dynamic_update_slice(spread, part, (0, j * tok // 2, 0))
    v.update(far_h=far_h, there=there, spread=spread)
    sync()

    parts = summed([v["sums"][0], v["far_h"], v["there"]])
    parts = [parts[k * rows : (k + 1) * rows] for k in range(4)]
    parts = [parts[0], z_down(parts[1]), z_far(parts[2]), z_up(parts[3])]
    ffn_other = y_swap(v["ffn_sum"])
    v.update(parts=parts)
    sync()

    attn_sum = summed(v["parts"], None, F32)
    vector = v["vector"] + lax.ppermute(v["vector"], "tp", Z_NEAR)
    v.update(attn_sum=attn_sum, vector=vector)
    v.update(ffn_other=ffn_other)
    sync()

    def finish(own, other):
        return jnp.concatenate(
            [jnp.where(ctx == 0, own, other), jnp.where(ctx == 0, other, own)], axis=0
        )

    def columns(first):
        parts = [ffn_grad[:, first(j) : first(j) + third] for j in range(3)]
        return jnp.concatenate(
            [
                jnp.where(ctx == 0, parts[0], parts[2]),
                parts[1],
                jnp.where(ctx == 0, parts[2], parts[0]),
            ],
            axis=1,
        )

    attn_other = y_swap(v["attn_sum"])
    vector = v["vector"] + lax.ppermute(v["vector"], "tp", Z_FAR)
    third = units // 3
    ffn_grad = finish(v["ffn_sum"], turn_chunks(v["ffn_other"]))
    grad_gate = columns(lambda j: 2 * j * third)
    grad_up = columns(lambda j: (2 * j + 1) * third)
    grad_down = columns(lambda j: 2 * units + j * third).T
    grad = jnp.zeros((rows_dev, tok, width), F32)
    grad = lax.dynamic_update_slice(grad, gathered[0].astype(F32), (0, 0, 0))
    v.update(vector=vector, attn_other=attn_other, grad=grad)
    v.update(grad_gate=grad_gate, grad_up=grad_up, grad_down=grad_down)
    sync()

    tokens_grad = lax.dynamic_update_slice(v["grad"], gathered[1].astype(F32), (0, tok // 2, 0))
    sums_all = v["vector"][0]

    attn_grad = finish(v["attn_sum"], v["attn_other"])
    teacher_loss = sums_all[2 * width + 2 * hd] / (v["total_count"] * width)

    def own_part(at, size):
        return lax.dynamic_slice_in_dim(sums_all, at + fsdp * (size // 4), size // 4, 0)

    return (
        v["spread"],
        teacher_loss,
        tokens_grad,
        own_part(0, width),
        attn_grad[:, :q_cols],
        attn_grad[:, q_cols : q_cols + k_cols],
        attn_grad[:, q_cols + k_cols : proj],
        own_part(2 * width, hd),
        own_part(2 * width + hd, hd),
        attn_grad[:, proj:].T,
        own_part(width, width),
        v["grad_gate"],
        v["grad_up"],
        v["grad_down"],
    )


def solution(mesh):
    return jax.shard_map(
        per_device_rows if fits(mesh) else per_device_any,
        mesh=mesh,
        in_specs=(
            P("fsdp", "ctx", None),
            P("fsdp", "ctx", None),
            P("fsdp"),
            P("fsdp"),
            P("fsdp", "tp"),
            P("fsdp", "tp"),
            P("fsdp", "tp"),
            P("fsdp"),
            P("fsdp"),
            P("tp", "fsdp"),
            P("fsdp"),
            P("fsdp", "tp"),
            P("fsdp", "tp"),
            P("tp", "fsdp"),
        ),
        out_specs=(
            P("fsdp", "ctx", None),
            P(),
            P("fsdp", "ctx", None),
            P("fsdp"),
            P("fsdp", "tp"),
            P("fsdp", "tp"),
            P("fsdp", "tp"),
            P("fsdp"),
            P("fsdp"),
            P("tp", "fsdp"),
            P("fsdp"),
            P("fsdp", "tp"),
            P("fsdp", "tp"),
            P("tp", "fsdp"),
        ),
        check_vma=False,
    )
```

```python
import functools
import math

import jax
import jax.numpy as jnp
from jax import lax
from jax.experimental import pallas as pl
from jax.experimental.pallas import tpu as pltpu
from jax.sharding import PartitionSpec as P

EPS = 1e-05
THETA = 1000000.0
NEGATIVE = -1e30


def rms_scale(field_in, gain_vec):
    return (
        field_in * lax.rsqrt(jnp.mean(field_in * field_in, axis=-1, keepdims=True) + EPS) * gain_vec
    )


def rotate(field_in, positions):
    half_dim = field_in.shape[-1] // 2
    frequency = THETA ** (-(2.0 * jnp.arange(half_dim, dtype=jnp.float32)) / field_in.shape[-1])
    angles = positions[:, None] * frequency[None, :]
    cos_part = jnp.cos(angles)[:, None, :]
    sin_part = jnp.sin(angles)[:, None, :]
    lower_half = field_in[..., :half_dim]
    upper_half = field_in[..., half_dim:]
    return jnp.concatenate(
        [
            lower_half * cos_part - upper_half * sin_part,
            upper_half * cos_part + lower_half * sin_part,
        ],
        axis=-1,
    )


def linear(left_mat, right_mat):
    return jnp.dot(left_mat, right_mat, preferred_element_type=jnp.float32)


def linear_left(left_mat, right_mat):
    return lax.dot_general(
        left_mat, right_mat, (((0,), (0,)), ((), ())), preferred_element_type=jnp.float32
    )


def linear_right(left_mat, right_mat):
    return lax.dot_general(
        left_mat, right_mat, (((1,), (1,)), ((), ())), preferred_element_type=jnp.float32
    )


def swiglu(gate_act, up_act):
    return jax.nn.silu(gate_act) * up_act


def per_device_any(
    tokens,
    teacher,
    lengths,
    attn_gain,
    q_weight,
    k_weight,
    v_weight,
    q_gain,
    k_gain,
    o_weight,
    ffn_gain,
    gate_weight,
    up_weight,
    down_weight,
):
    (
        gain_one,
        w_query,
        w_key,
        w_value,
        gain_query,
        gain_key,
        w_output,
        gain_two,
        w_gate,
        w_upper,
        w_down,
    ) = (
        lax.all_gather(attn_gain, "fsdp", axis=0, tiled=True),
        lax.all_gather(q_weight, "fsdp", axis=0, tiled=True),
        lax.all_gather(k_weight, "fsdp", axis=0, tiled=True),
        lax.all_gather(v_weight, "fsdp", axis=0, tiled=True),
        lax.all_gather(q_gain, "fsdp", axis=0, tiled=True),
        lax.all_gather(k_gain, "fsdp", axis=0, tiled=True),
        lax.all_gather(o_weight, "fsdp", axis=1, tiled=True),
        lax.all_gather(ffn_gain, "fsdp", axis=0, tiled=True),
        lax.all_gather(gate_weight, "fsdp", axis=0, tiled=True),
        lax.all_gather(up_weight, "fsdp", axis=0, tiled=True),
        lax.all_gather(down_weight, "fsdp", axis=1, tiled=True),
    )
    rows_dev, block_len, model_width = tokens.shape
    count_tok = rows_dev * block_len
    head_dim = gain_query.shape[0]
    q_heads = w_query.shape[1] // head_dim
    kv_heads = w_key.shape[1] // head_dim
    group_size = q_heads // kv_heads
    score_scale = head_dim ** (-0.5)
    row_len = block_len * lax.axis_size("ctx")
    key_block = math.gcd(row_len, 512)
    block_start = lax.axis_index("ctx") * block_len
    tiles_used = (block_start + block_len + key_block - 1) // key_block
    slot_pos = block_start + jnp.arange(block_len, dtype=jnp.int32)
    positions = slot_pos.astype(jnp.float32)
    valid = (slot_pos[None, :] < lengths[:, None]).astype(jnp.float32)
    slots = count_tok * lax.axis_size("fsdp") * lax.axis_size("ctx")
    gain_two_f = gain_two.astype(jnp.float32)
    gain_one_f = gain_one.astype(jnp.float32)
    inputs = tokens.astype(jnp.float32)
    normed_one, back_one = jax.vjp(rms_scale, inputs, gain_one_f)
    normed_low = normed_one.astype(jnp.bfloat16).reshape(count_tok, model_width)
    query_raw = linear(normed_low, w_query)
    key_raw = linear(normed_low, w_key)
    value_raw = linear(normed_low, w_value)

    def heads_post(raw_heads, gain_vec):
        shaped = raw_heads.reshape(rows_dev, block_len, -1, head_dim)
        return rotate(rms_scale(shaped, gain_vec), positions)

    query_rot, query_back = jax.vjp(heads_post, query_raw, gain_query.astype(jnp.float32))
    key_rot, key_back = jax.vjp(heads_post, key_raw, gain_key.astype(jnp.float32))
    queries = query_rot.astype(jnp.bfloat16).reshape(
        rows_dev, block_len, kv_heads, group_size, head_dim
    )
    key_rows = key_rot.astype(jnp.bfloat16).reshape(rows_dev, block_len, kv_heads * head_dim)
    values = value_raw.astype(jnp.bfloat16).reshape(rows_dev, block_len, kv_heads * head_dim)
    keys_all, values_all = (
        lax.all_gather(key_rows, "ctx", axis=1, tiled=True),
        lax.all_gather(values, "ctx", axis=1, tiled=True),
    )

    def key_tile(tile_index):
        tile_start = tile_index * key_block
        key_pos = tile_start + jnp.arange(key_block, dtype=jnp.int32)
        key_part = lax.dynamic_slice_in_dim(keys_all, tile_start, key_block, 1).reshape(
            rows_dev, key_block, kv_heads, head_dim
        )
        value_part = lax.dynamic_slice_in_dim(values_all, tile_start, key_block, 1).reshape(
            rows_dev, key_block, kv_heads, head_dim
        )
        scores = (
            jnp.einsum("rqhgd,rkhd->rhgqk", queries, key_part, preferred_element_type=jnp.float32)
            * score_scale
        )
        allowed = (key_pos[None, None, :] <= slot_pos[None, :, None]) & (
            key_pos[None, None, :] < lengths[:, None, None]
        )
        return (tile_start, scores, allowed[:, None, None], key_part, value_part)

    stat_shape = (rows_dev, kv_heads, group_size, block_len)

    def stats_step(tile_index, carried):
        running_max, running_sum = carried
        tile_start, scores, allowed, key_part, value_part = key_tile(tile_index)
        masked = jnp.where(allowed, scores, NEGATIVE)
        new_max = jnp.maximum(running_max, jnp.max(masked, axis=-1))
        terms = jnp.where(allowed, jnp.exp(masked - new_max[..., None]), 0.0)
        return (new_max, running_sum * jnp.exp(running_max - new_max) + jnp.sum(terms, axis=-1))

    running_max, running_sum = lax.fori_loop(
        0,
        tiles_used,
        stats_step,
        (jnp.full(stat_shape, NEGATIVE, jnp.float32), jnp.zeros(stat_shape, jnp.float32)),
    )
    log_total = running_max + jnp.log(running_sum)
    out_shape = (rows_dev, block_len, kv_heads, group_size, head_dim)

    def value_step(tile_index, carried):
        rounded_out, exact_out = carried
        tile_start, scores, allowed, key_part, value_part = key_tile(tile_index)
        tile_probs = jnp.where(allowed, jnp.exp(scores - log_total[..., None]), 0.0)
        rounded_out = rounded_out + jnp.einsum(
            "rhgqk,rkhd->rqhgd",
            tile_probs.astype(jnp.bfloat16),
            value_part,
            preferred_element_type=jnp.float32,
        )
        exact_out = exact_out + jnp.einsum(
            "rhgqk,rkhd->rqhgd", tile_probs, value_part.astype(jnp.float32)
        )
        return (rounded_out, exact_out)

    rounded_out, exact_out = lax.fori_loop(
        0,
        tiles_used,
        value_step,
        (jnp.zeros(out_shape, jnp.float32), jnp.zeros(out_shape, jnp.float32)),
    )
    attended = rounded_out.astype(jnp.bfloat16).reshape(count_tok, q_heads * head_dim)
    attn_total = lax.psum(linear(attended, w_output), "tp")
    resid = inputs + attn_total.reshape(rows_dev, block_len, model_width)
    normed_two, back_two = jax.vjp(rms_scale, resid, gain_two_f)
    normed_second = normed_two.astype(jnp.bfloat16).reshape(count_tok, model_width)
    gate_act = linear(normed_second, w_gate)
    up_act = linear(normed_second, w_upper)
    hidden_full, back_glu = jax.vjp(swiglu, gate_act, up_act)
    hidden = hidden_full.astype(jnp.bfloat16)
    ffn_total = lax.psum(linear(hidden, w_down), "tp")
    result = resid + ffn_total.reshape(rows_dev, block_len, model_width)
    error_value = result - teacher.astype(jnp.float32)
    valid_col = valid[..., None]
    total_square, total_count = lax.psum(
        (jnp.sum(valid_col * error_value * error_value), jnp.sum(valid)), ("fsdp", "ctx")
    )
    teacher_loss = total_square / (total_count * model_width)
    grad_result = valid_col * error_value * (slots / total_count)
    grad_low = grad_result.astype(jnp.bfloat16).reshape(count_tok, model_width)
    grad_down = linear_left(hidden, grad_low)
    grad_hidden = linear_right(grad_low, w_down)
    grad_gate_full, grad_up_full = back_glu(grad_hidden)
    grad_gate = grad_gate_full.astype(jnp.bfloat16)
    grad_up = grad_up_full.astype(jnp.bfloat16)
    grad_wgate = linear_left(normed_second, grad_gate)
    grad_wup = linear_left(normed_second, grad_up)
    normed_two_part = linear_right(grad_gate, w_gate) + linear_right(grad_up, w_upper)
    grad_normed_two = lax.psum(normed_two_part, "tp")
    grad_resid_norm, grad_gain_two = back_two(
        grad_normed_two.reshape(rows_dev, block_len, model_width)
    )
    grad_resid = grad_result + grad_resid_norm
    grad_attn_low = grad_resid.astype(jnp.bfloat16).reshape(count_tok, model_width)
    grad_woutput = linear_left(attended, grad_attn_low)
    grad_attended = linear_right(grad_attn_low, w_output).astype(jnp.bfloat16).reshape(out_shape)
    delta = jnp.einsum("rqhgd,rqhgd->rhgq", grad_attended.astype(jnp.float32), exact_out)
    full_shape = (rows_dev, row_len, kv_heads * head_dim)

    def grad_step(tile_index, carried):
        grad_queries, grad_keys, grad_values = carried
        tile_start, scores, allowed, key_part, value_part = key_tile(tile_index)
        tile_probs = jnp.where(allowed, jnp.exp(scores - log_total[..., None]), 0.0)
        grad_probs = jnp.einsum(
            "rqhgd,rkhd->rhgqk", grad_attended, value_part, preferred_element_type=jnp.float32
        )
        grad_scores = (tile_probs * (grad_probs - delta[..., None])).astype(jnp.bfloat16)
        grad_queries = (
            grad_queries
            + jnp.einsum(
                "rhgqk,rkhd->rqhgd", grad_scores, key_part, preferred_element_type=jnp.float32
            )
            * score_scale
        )
        key_term = (
            jnp.einsum(
                "rhgqk,rqhgd->rkhd", grad_scores, queries, preferred_element_type=jnp.float32
            )
            * score_scale
        )
        value_term = jnp.einsum(
            "rhgqk,rqhgd->rkhd",
            tile_probs.astype(jnp.bfloat16),
            grad_attended,
            preferred_element_type=jnp.float32,
        )
        grad_keys = lax.dynamic_update_slice_in_dim(
            grad_keys, key_term.reshape(rows_dev, key_block, kv_heads * head_dim), tile_start, 1
        )
        grad_values = lax.dynamic_update_slice_in_dim(
            grad_values, value_term.reshape(rows_dev, key_block, kv_heads * head_dim), tile_start, 1
        )
        return (grad_queries, grad_keys, grad_values)

    grad_queries, grad_keys, grad_values = lax.fori_loop(
        0,
        tiles_used,
        grad_step,
        (
            jnp.zeros(out_shape, jnp.float32),
            jnp.zeros(full_shape, jnp.float32),
            jnp.zeros(full_shape, jnp.float32),
        ),
    )
    key_grad, value_grad = (
        lax.psum_scatter(grad_keys, "ctx", scatter_dimension=1, tiled=True),
        lax.psum_scatter(grad_values, "ctx", scatter_dimension=1, tiled=True),
    )
    grad_query_raw, grad_gain_query = query_back(
        grad_queries.reshape(rows_dev, block_len, q_heads, head_dim)
    )
    grad_key_raw, grad_gain_key = key_back(
        key_grad.reshape(rows_dev, block_len, kv_heads, head_dim)
    )
    query_low = grad_query_raw.astype(jnp.bfloat16)
    key_low = grad_key_raw.astype(jnp.bfloat16)
    value_low = value_grad.reshape(count_tok, kv_heads * head_dim).astype(jnp.bfloat16)
    grad_wquery = linear_left(normed_low, query_low)
    grad_wkey = linear_left(normed_low, key_low)
    grad_wvalue = linear_left(normed_low, value_low)
    normed_part = (
        linear_right(query_low, w_query)
        + linear_right(key_low, w_key)
        + linear_right(value_low, w_value)
    )
    grad_normed_one, grad_gain_query, grad_gain_key = lax.psum(
        (normed_part, grad_gain_query, grad_gain_key), "tp"
    )
    grad_input_norm, grad_gain_one = back_one(
        grad_normed_one.reshape(rows_dev, block_len, model_width)
    )
    tokens_grad = grad_resid + grad_input_norm
    partials = (
        grad_gain_one,
        grad_wquery,
        grad_wkey,
        grad_wvalue,
        grad_gain_query,
        grad_gain_key,
        grad_woutput,
        grad_gain_two,
        grad_wgate,
        grad_wup,
        grad_down,
    )
    pieces = (
        lax.psum_scatter(partials[0], ("fsdp", "ctx"), scatter_dimension=0, tiled=True),
        lax.psum_scatter(partials[1], ("fsdp", "ctx"), scatter_dimension=0, tiled=True),
        lax.psum_scatter(partials[2], ("fsdp", "ctx"), scatter_dimension=0, tiled=True),
        lax.psum_scatter(partials[3], ("fsdp", "ctx"), scatter_dimension=0, tiled=True),
        lax.psum_scatter(partials[4], ("fsdp", "ctx"), scatter_dimension=0, tiled=True),
        lax.psum_scatter(partials[5], ("fsdp", "ctx"), scatter_dimension=0, tiled=True),
        lax.psum_scatter(partials[6], ("fsdp", "ctx"), scatter_dimension=1, tiled=True),
        lax.psum_scatter(partials[7], ("fsdp", "ctx"), scatter_dimension=0, tiled=True),
        lax.psum_scatter(partials[8], ("fsdp", "ctx"), scatter_dimension=0, tiled=True),
        lax.psum_scatter(partials[9], ("fsdp", "ctx"), scatter_dimension=0, tiled=True),
        lax.psum_scatter(partials[10], ("fsdp", "ctx"), scatter_dimension=1, tiled=True),
    )
    summed = (
        lax.all_gather(pieces[0], "ctx", axis=0, tiled=True),
        lax.all_gather(pieces[1], "ctx", axis=0, tiled=True),
        lax.all_gather(pieces[2], "ctx", axis=0, tiled=True),
        lax.all_gather(pieces[3], "ctx", axis=0, tiled=True),
        lax.all_gather(pieces[4], "ctx", axis=0, tiled=True),
        lax.all_gather(pieces[5], "ctx", axis=0, tiled=True),
        lax.all_gather(pieces[6], "ctx", axis=1, tiled=True),
        lax.all_gather(pieces[7], "ctx", axis=0, tiled=True),
        lax.all_gather(pieces[8], "ctx", axis=0, tiled=True),
        lax.all_gather(pieces[9], "ctx", axis=0, tiled=True),
        lax.all_gather(pieces[10], "ctx", axis=1, tiled=True),
    )
    return (
        result.astype(jnp.bfloat16),
        teacher_loss,
        tokens_grad,
        summed[0],
        summed[1],
        summed[2],
        summed[3],
        summed[4],
        summed[5],
        summed[6],
        summed[7],
        summed[8],
        summed[9],
        summed[10],
    )


BF16 = jnp.bfloat16
F32 = jnp.float32
LOG2E = math.log2(math.e)
X_SWAP = [(0, 2), (2, 0), (1, 3), (3, 1)]
CORE_SWAP = [(0, 1), (1, 0), (2, 3), (3, 2)]
Y_SWAP = [(0, 1), (1, 0)]
Z_UP = [(0, 1), (1, 2), (2, 3), (3, 0)]
Z_DOWN = [(0, 3), (1, 0), (2, 1), (3, 2)]
Z_NEAR = [(0, 1), (1, 0), (2, 3), (3, 2)]
Z_FAR = [(0, 2), (2, 0), (1, 3), (3, 1)]
MASKS = (0, 2, 1, 3)
ANY = pl.BlockSpec(memory_space=pl.ANY)
SMEM = pl.BlockSpec(memory_space=pltpu.SMEM)


def fits(mesh):
    return dict(mesh.shape) == {"fsdp": 4, "ctx": 2, "tp": 4}


def dot(left, right, left_dim, right_dim):
    return lax.dot_general(
        left, right, (((left_dim,), (right_dim,)), ((), ())), preferred_element_type=F32
    )


def sigmoid(v):
    return 0.5 * jnp.tanh(0.5 * v) + 0.5


def whole(shape):
    zeros = (0,) * len(shape)
    return pl.BlockSpec(shape, lambda *_: zeros, pipeline_mode=pl.Buffered(1))


def settings(dims, mib):
    return pltpu.CompilerParams(
        dimension_semantics=("arbitrary",) * dims, vmem_limit_bytes=mib << 20
    )


def shape_of(shape, dtype):
    return jax.ShapeDtypeStruct(shape, dtype)


def cost(large, microseconds=None):
    size = 1 << 42 if large else 1 << 10
    if microseconds is not None:
        size = int(microseconds * 1.15e9)
    return pl.CostEstimate(flops=size, bytes_accessed=size >> 12, transcendentals=0)


def pack_kernel(info, o_in, g_in, u_in, d_in, *refs):
    out_ref, ffn_ref, *chunk_refs, others_ref, o_ref, g_ref, u_ref, d_ref, sems = refs
    ctx = info[2]
    pairs = ((o_in, o_ref), (g_in, g_ref), (u_in, u_ref), (d_in, d_ref))
    copies = [pltpu.make_async_copy(a, b, sems.at[i]) for i, (a, b) in enumerate(pairs)]
    for copy in copies:
        copy.start()
    for copy in copies:
        copy.wait()
    out_ref[...] = o_ref[...].astype(F32).T.astype(BF16)
    third = g_ref.shape[1] // 3
    for j in range(3):
        at = pl.multiple_of(jnp.where(ctx == 0, j, 2 - j) * third, third)
        parts = [
            g_ref[:, pl.ds(at, third)],
            u_ref[:, pl.ds(at, third)],
            d_ref[pl.ds(at, third), :].astype(F32).T.astype(BF16),
        ]
        for i, part in enumerate(parts):
            chunk_refs[j][:, i * third : (i + 1) * third] = part
            if j:
                others_ref[:, (3 * j - 3 + i) * third : (3 * j - 2 + i) * third] = part
            ffn_ref[:, (3 * j + i) * third : (3 * j + i + 1) * third] = part


def pack(info, o, g, u, d):
    rows, units = g.shape
    feats = o.shape[0]
    widths = (feats, 3 * units, units, units, units, 2 * units)
    return pl.pallas_call(
        pack_kernel,
        in_specs=[SMEM] + [ANY] * 4,
        out_specs=[pl.BlockSpec(memory_space=pltpu.VMEM)] * 6,
        out_shape=[shape_of((rows, n), BF16) for n in widths],
        scratch_shapes=[pltpu.VMEM(a.shape, BF16) for a in (o, g, u, d)]
        + [pltpu.SemaphoreType.DMA((4,))],
        compiler_params=pltpu.CompilerParams(vmem_limit_bytes=24 << 20),
        cost_estimate=cost(False),
        name="pack",
    )(info, o, g, u, d)


def join_kernel(q_ref, k_ref, v_ref, out_ref):
    at = 0
    for ref in (q_ref, k_ref, v_ref):
        out_ref[:, at : at + ref.shape[1]] = ref[...]
        at += ref.shape[1]


def join(q, k, v):
    return pl.pallas_call(
        join_kernel,
        out_shape=shape_of((q.shape[0], q.shape[1] + k.shape[1] + v.shape[1]), BF16),
        compiler_params=pltpu.CompilerParams(vmem_limit_bytes=8 << 20),
        cost_estimate=cost(False),
        name="join",
    )(q, k, v)


def norm_one_kernel(info, tok_ref, gain_ref, x_ref, nt_ref, x32):
    quarter = x_ref.shape[1] // 4
    for p, mask in enumerate(MASKS):
        at = pl.multiple_of(jnp.bitwise_xor(info[1], mask) * quarter, quarter)
        part = tok_ref[0, :, pl.ds(at, quarter)]
        x_ref[:, p * quarter : (p + 1) * quarter] = part
        x32[:, p * quarter : (p + 1) * quarter] = part.astype(F32)
    x = x32[...]
    rho = lax.rsqrt(jnp.mean(x * x, axis=-1, keepdims=True) + EPS)
    nt_ref[...] = (x * rho * gain_ref[...]).T.astype(BF16)


def norm_one(info, tokens, gain, tile):
    _, tok, width = tokens.shape
    return pl.pallas_call(
        norm_one_kernel,
        grid_spec=pltpu.PrefetchScalarGridSpec(
            num_scalar_prefetch=1,
            grid=(tok // tile,),
            in_specs=[
                pl.BlockSpec((1, tile, width), lambda i, info: (info[0], i, 0)),
                pl.BlockSpec((1, width), lambda i, info: (0, 0)),
            ],
            out_specs=[
                pl.BlockSpec((tile, width), lambda i, info: (i, 0)),
                pl.BlockSpec((width, tile), lambda i, info: (0, i)),
            ],
            scratch_shapes=[pltpu.VMEM((tile, width), F32)],
        ),
        out_shape=[shape_of((tok, width), BF16), shape_of((width, tok), BF16)],
        compiler_params=settings(1, 24),
        cost_estimate=cost(False),
        name="norm_one",
    )(info, tokens, gain)


def proj_kernel(heads, block, plan, count, info, *refs):
    nt_ref, cos_ref, sin_ref, qg_ref, kg_ref, rot_ref, raw_ref, w_ref, sem = refs[count:]
    rows = w_ref.shape[0] // 4

    @pl.when(pl.program_id(0) == 0)
    def _():
        for k in range(4):

            @pl.when(block(info) == k)
            def _():
                for p, (piece, row) in enumerate(plan[k]):
                    src = refs[piece].at[pl.ds(row, rows)]
                    pltpu.make_async_copy(src, w_ref.at[pl.ds(p * rows, rows)], sem).start()

        pltpu.make_async_copy(w_ref, w_ref, sem).wait()

    hd = qg_ref.shape[0]
    half = hd // 2
    raw = dot(w_ref[...], nt_ref[...], 0, 0)
    cos_part, sin_part = cos_ref[...], sin_ref[...]
    heads_q, heads_k = heads
    raw_ref[...] = raw.astype(BF16)
    for h in range(heads_q + heads_k):
        v = raw[h * hd : (h + 1) * hd]
        rho = lax.rsqrt(jnp.mean(v * v, axis=0, keepdims=True) + EPS)
        v = v * rho * (qg_ref[...] if h < heads_q else kg_ref[...])
        a, b = v[:half], v[half:]
        rot_ref[h * hd : h * hd + half, :] = (a * cos_part - b * sin_part).astype(BF16)
        rot_ref[h * hd + half : (h + 1) * hd, :] = (b * cos_part + a * sin_part).astype(BF16)
    at = (heads_q + heads_k) * hd
    rot_ref[at:, :] = raw[at:].astype(BF16)


def project(info, weights, normed_t, cos_part, sin_part, gain_q, gain_k, heads, block):
    plan, pieces = weights
    width, tok = normed_t.shape
    cols = pieces[0].shape[1]
    tile = min(512, tok)
    const = lambda a: pl.BlockSpec(a.shape, lambda i, info: (0, 0))
    tab = lambda a: pl.BlockSpec((a.shape[0], tile), lambda i, info: (0, i))
    return pl.pallas_call(
        functools.partial(proj_kernel, heads, block, plan, len(pieces)),
        grid_spec=pltpu.PrefetchScalarGridSpec(
            num_scalar_prefetch=1,
            grid=(tok // tile,),
            in_specs=[ANY] * len(pieces)
            + [tab(normed_t), tab(cos_part), tab(sin_part), const(gain_q), const(gain_k)],
            out_specs=[pl.BlockSpec((cols, tile), lambda i, info: (0, i))] * 2,
            scratch_shapes=[pltpu.VMEM((width, cols), BF16), pltpu.SemaphoreType.DMA],
        ),
        out_shape=[shape_of((cols, tok), BF16), shape_of((cols, tok), BF16)],
        compiler_params=settings(1, 24),
        cost_estimate=cost(False),
        name="project",
    )(info, *pieces, normed_t, cos_part, sin_part, gain_q, gain_k)


def head_back_kernel(
    heads, info, dm_ref, dt_ref, rm_ref, rt_ref, cos_ref, sin_ref, qg_ref, kg_ref, out_ref, gg_ref
):
    step, part = pl.program_id(0), pl.program_id(1)
    hd = qg_ref.shape[0]
    half = hd // 2
    heads_q, heads_k = heads
    cos_part, sin_part = cos_ref[...], sin_ref[...]
    tile = cos_part.shape[1]

    @pl.when((step == 0) & (part == 0))
    def _():
        gg_ref[...] = jnp.zeros_like(gg_ref)

    def work(d_ref, r_ref):
        gain_q = jnp.zeros((hd, 1), F32)
        gain_k = jnp.zeros((hd, 1), F32)
        done = []
        for h in range(heads_q + heads_k):
            is_q = h < heads_q
            g = d_ref[h * hd : (h + 1) * hd, :].astype(F32)
            raw = r_ref[h * hd : (h + 1) * hd, :].astype(F32)
            a, b = g[:half], g[half:]
            turned = jnp.concatenate(
                [a * cos_part + b * sin_part, b * cos_part - a * sin_part], axis=0
            )
            rho = lax.rsqrt(jnp.mean(raw * raw, axis=0, keepdims=True) + EPS)
            unit = raw * rho
            prod = turned * unit
            scaled = turned * (qg_ref[...] if is_q else kg_ref[...])
            mean = jnp.mean(scaled * unit, axis=0, keepdims=True)
            done.append(rho * (scaled - unit * mean))
            total = jnp.sum(prod, axis=1, keepdims=True)
            if is_q:
                gain_q = gain_q + total
            else:
                gain_k = gain_k + total
        done.append(d_ref[(heads_q + heads_k) * hd :, :].astype(F32))
        out_ref[0] = jnp.concatenate(done, axis=0).T.astype(BF16)
        lane = lax.broadcasted_iota(jnp.int32, gg_ref.shape, 1)
        gg_ref[...] += jnp.where(lane == 0, gain_q, jnp.where(lane == 1, gain_k, 0.0))

    @pl.when(step == 0)
    def _():
        work(dm_ref, rm_ref)

    @pl.when(step == 1)
    def _():
        work(dt_ref, rt_ref)


def head_back(info, grad_mine, grad_theirs, raw_mine, raw_theirs, cos_part, sin_part, gq, gk, heads):
    cols, tok = grad_mine.shape
    tile = min(512, tok)
    mine = pl.BlockSpec((cols, tile), lambda s, i, info: (0, jnp.where(s == 0, i, tok // tile - 1)))
    theirs = pl.BlockSpec((cols, tile), lambda s, i, info: (0, jnp.where(s == 0, 0, i)))
    tab = lambda a: pl.BlockSpec((a.shape[0], tile), lambda s, i, info: (0, i))
    const = lambda a: pl.BlockSpec(a.shape, lambda s, i, info: (0, 0))
    return pl.pallas_call(
        functools.partial(head_back_kernel, heads),
        grid_spec=pltpu.PrefetchScalarGridSpec(
            num_scalar_prefetch=1,
            grid=(2, tok // tile),
            in_specs=[
                mine,
                theirs,
                mine,
                theirs,
                tab(cos_part),
                tab(sin_part),
                const(gq),
                const(gk),
            ],
            out_specs=[
                pl.BlockSpec(
                    (1, tile, cols), lambda s, i, info: (jnp.bitwise_xor(info[2], s), i, 0)
                ),
                pl.BlockSpec((gq.shape[0], 128), lambda s, i, info: (0, 0)),
            ],
        ),
        out_shape=[shape_of((2, tok, cols), BF16), shape_of((gq.shape[0], 128), F32)],
        compiler_params=settings(2, 60),
        cost_estimate=cost(False),
        name="head_back",
    )(info, grad_mine, grad_theirs, raw_mine, raw_theirs, cos_part, sin_part, gq, gk)


def load_rows(info, mine_ref, got_ref, rows, sems):
    tok = mine_ref.shape[1]
    ctx = info[2]
    here = pl.multiple_of(ctx * tok, tok)
    there = pl.multiple_of((1 - ctx) * tok, tok)
    one = pltpu.make_async_copy(mine_ref, rows.at[:, pl.ds(here, tok)], sems.at[0])
    two = pltpu.make_async_copy(got_ref, rows.at[:, pl.ds(there, tok)], sems.at[1])
    one.start()
    two.start()
    one.wait()
    two.wait()


def keys_with_bias(keys, length):
    hd, slots = keys.shape
    pos = lax.broadcasted_iota(jnp.int32, (hd, slots), 1)
    row = lax.broadcasted_iota(jnp.int32, (hd, slots), 0)
    bias = jnp.where((row == 0) & (pos >= length), NEGATIVE, 0.0)
    return jnp.concatenate([keys.astype(F32), bias], axis=0).T.astype(BF16)


def query_with_one(pair):
    one_row = jnp.where(lax.broadcasted_iota(jnp.int32, pair.shape, 0) == 0, 1.0, 0.0)
    return jnp.concatenate([pair, one_row.astype(BF16)], axis=0)


def by_halves(left, right):
    half = left.shape[1] // 2
    return jnp.concatenate(
        [left[:, :half], right[:, :half], left[:, half:], right[:, half:]], axis=1
    )


def by_heads(both):
    quarter = both.shape[1] // 4
    part = lambda i: both[:, i * quarter : (i + 1) * quarter]
    return (
        jnp.concatenate([part(0), part(2)], axis=1),
        jnp.concatenate([part(1), part(3)], axis=1),
    )


def causal(scores):
    half = scores.shape[0]
    key_pos = lax.broadcasted_iota(jnp.int32, (half, half), 0)
    query_pos = lax.broadcasted_iota(jnp.int32, (half, half), 1)
    allowed = key_pos <= query_pos
    return jnp.where(jnp.concatenate([allowed, allowed], axis=1), scores, NEGATIVE)


def attn_fwd_kernel(
    width, hd, info, mine_ref, got_ref, keep_ref, send_ref, lse_ref, rows, key_rows, sems
):
    head, block = pl.program_id(0), pl.program_id(1)
    heads_k = pl.num_programs(0)
    scale = hd**-0.5 * LOG2E
    length = info[3]
    key_at = pl.multiple_of(heads_k * 2 * hd + head * hd, hd)
    value_at = pl.multiple_of(heads_k * 3 * hd + head * hd, hd)
    query_at = pl.multiple_of(head * 2 * hd, 2 * hd)

    @pl.when((head == 0) & (block == 0))
    def _():
        load_rows(info, mine_ref, got_ref, rows, sems)

    @pl.when(block == 0)
    def _():
        key_rows[...] = keys_with_bias(rows[pl.ds(key_at, hd), :], length)

    start = pl.multiple_of(block * width, width)
    both = rows[pl.ds(query_at, 2 * hd), pl.ds(start, width)]
    query = query_with_one(by_halves(both[:hd], both[hd:]))

    def tile(at, carried, diagonal):
        out, total = carried
        scores = dot(key_rows[pl.ds(at, width), :], query, 1, 0)
        if diagonal:
            key_pos = lax.broadcasted_iota(jnp.int32, (width, width), 0)
            query_pos = lax.broadcasted_iota(jnp.int32, (width, width), 1)
            allowed = key_pos <= query_pos
            allowed = by_halves(allowed, allowed)
            scores = jnp.where(allowed, scores, NEGATIVE)
        probs = jnp.exp2(scores * scale)
        total = total + jnp.sum(probs, axis=0, keepdims=True)
        out = out + dot(rows[pl.ds(value_at, hd), pl.ds(at, width)], probs.astype(BF16), 1, 0)
        return out, total

    carried = (jnp.zeros((hd, 2 * width), F32), jnp.zeros((1, 2 * width), F32))
    full = jnp.minimum(block, lax.div(length + width - 1, width))
    carried = lax.fori_loop(
        0, full, lambda j, c: tile(pl.multiple_of(j * width, width), c, False), carried
    )
    out, total = tile(start, carried, True)
    out = out * (1.0 / total)
    out = jnp.concatenate(by_heads(out), axis=0).T.astype(BF16)
    here = block // 2 == info[2]

    @pl.when(here)
    def _():
        keep_ref[...] = out

    @pl.when(jnp.logical_not(here))
    def _():
        send_ref[...] = out

    log_first, log_second = by_heads(jnp.log2(total))
    lse_ref[0, 0:1, :] = log_first
    lse_ref[0, 1:2, :] = log_second


def keep_block(i, info):
    return jnp.clip(i - 2 * info[2], 0, 1)


def send_block(i, info):
    return jnp.clip(i - 2 * (1 - info[2]), 0, 1)


def attn_fwd(info, mine, got, hd):
    cols, tok = mine.shape
    heads_k = cols // (4 * hd)
    width = tok // 2
    return pl.pallas_call(
        functools.partial(attn_fwd_kernel, width, hd),
        grid_spec=pltpu.PrefetchScalarGridSpec(
            num_scalar_prefetch=1,
            grid=(heads_k, 4),
            in_specs=[ANY, ANY],
            out_specs=[
                pl.BlockSpec((width, 2 * hd), lambda h, i, info: (keep_block(i, info), h)),
                pl.BlockSpec((width, 2 * hd), lambda h, i, info: (send_block(i, info), h)),
                pl.BlockSpec((1, 2, width), lambda h, i, info: (h, 0, i)),
            ],
            scratch_shapes=[
                pltpu.VMEM((cols, 2 * tok), BF16),
                pltpu.VMEM((2 * tok, 2 * hd), BF16),
                pltpu.SemaphoreType.DMA((2,)),
            ],
        ),
        out_shape=[
            shape_of((tok, heads_k * 2 * hd), BF16),
            shape_of((tok, heads_k * 2 * hd), BF16),
            shape_of((heads_k, 2, 2 * tok), F32),
        ],
        compiler_params=settings(2, 60),
        cost_estimate=cost(True),
        name="attn_fwd",
    )(info, mine, got)


def attn_bwd_kernel(
    width,
    hd,
    info,
    mine_ref,
    got_ref,
    ok_ref,
    os_ref,
    gk_ref,
    gs_ref,
    lse_ref,
    keep_ref,
    send_ref,
    rows,
    key_rows,
    value_rows,
    key_sum,
    value_sum,
    sems,
):
    head, block = pl.program_id(0), pl.program_id(1)
    heads_k = pl.num_programs(0)
    scale = hd**-0.5
    length = info[3]
    ctx = info[2]
    tok = keep_ref.shape[1]
    key_at = pl.multiple_of(heads_k * 2 * hd + head * hd, hd)
    value_at = pl.multiple_of(heads_k * 3 * hd + head * hd, hd)
    query_at = pl.multiple_of(head * 2 * hd, 2 * hd)

    @pl.when((head == 0) & (block == 0))
    def _():
        load_rows(info, mine_ref, got_ref, rows, sems)

    @pl.when(block == 0)
    def _():
        key_rows[...] = keys_with_bias(rows[pl.ds(key_at, hd), :], length)
        value_rows[...] = rows[pl.ds(value_at, hd), :].astype(F32).T.astype(BF16)
        key_sum[...] = jnp.zeros_like(key_sum)
        value_sum[...] = jnp.zeros_like(value_sum)

    start = pl.multiple_of(block * width, width)
    here = block // 2 == ctx

    def store_query(value):
        at = pl.ds(pl.multiple_of((block % 2) * width, width), width)

        @pl.when(here)
        def _():
            keep_ref[pl.ds(query_at, 2 * hd), at] = value

        @pl.when(jnp.logical_not(here))
        def _():
            send_ref[pl.ds(query_at, 2 * hd), at] = value

    @pl.when(block * width < length)
    def _():
        both = rows[pl.ds(query_at, 2 * hd), pl.ds(start, width)]
        pair = by_halves(both[:hd], both[hd:])
        query = query_with_one(pair)
        query_rows = pair.astype(F32).T.astype(BF16)
        grad_wide = jnp.where(here, gk_ref[...].astype(F32), gs_ref[...].astype(F32))
        out_wide = jnp.where(here, ok_ref[...].astype(F32), os_ref[...].astype(F32))
        grad_t = grad_wide.T
        prod = (grad_wide * out_wide).T
        grad = by_halves(grad_t[:hd], grad_t[hd:]).astype(BF16)
        half = width // 2
        grad_rows = jnp.concatenate(
            [
                grad_wide[:half, :hd],
                grad_wide[:half, hd:],
                grad_wide[half:, :hd],
                grad_wide[half:, hd:],
            ],
            axis=0,
        ).astype(BF16)
        delta = by_halves(
            jnp.sum(prod[:hd], axis=0, keepdims=True), jnp.sum(prod[hd:], axis=0, keepdims=True)
        )
        lse = by_halves(lse_ref[0, 0:1, :], lse_ref[0, 1:2, :])

        def terms(at, keys, first, mask):
            scores = dot(key_rows[pl.ds(at, keys), :], query[:, first:], 1, 0)
            if mask:
                part = causal(scores[:, :width])
                wide = scores.shape[1] > width
                scores = jnp.concatenate([part, scores[:, width:]], axis=1) if wide else part
            probs = jnp.exp2(scores * (scale * LOG2E) - lse[:, first:])
            grad_probs = dot(value_rows[pl.ds(at, keys), :], grad[:, first:], 1, 0)
            grad_scores = (probs * (grad_probs - delta[:, first:])).astype(BF16)
            value_sum[pl.ds(at, keys), :] += dot(probs.astype(BF16), grad_rows[first:], 1, 0)
            key_sum[pl.ds(at, keys), :] += dot(grad_scores, query_rows[first:], 1, 0)
            return dot(rows[pl.ds(key_at, hd), pl.ds(at, keys)], grad_scores, 1, 0)

        query_sum = lax.fori_loop(
            0,
            block,
            lambda j, s: s + terms(pl.multiple_of(j * width, width), width, 0, False),
            jnp.zeros((hd, 2 * width), F32),
        )
        query_sum = query_sum + terms(start, half, 0, True)
        later = terms(pl.multiple_of(start + half, half), half, width, True)
        query_sum = jnp.concatenate([query_sum[:, :width], query_sum[:, width:] + later], axis=1)
        store_query(jnp.concatenate(by_heads(query_sum * scale), axis=0).astype(BF16))

    @pl.when(block * width >= length)
    def _():
        store_query(jnp.zeros((2 * hd, width), BF16))

    @pl.when(block == 3)
    def _():
        for at, total in ((key_at, key_sum[...] * scale), (value_at, value_sum[...])):
            total = total.T.astype(BF16)
            left, right = total[:, :tok], total[:, tok:]

            @pl.when(ctx == 0)
            def _():
                keep_ref[pl.ds(at, hd), :] = left
                send_ref[pl.ds(at, hd), :] = right

            @pl.when(ctx == 1)
            def _():
                keep_ref[pl.ds(at, hd), :] = right
                send_ref[pl.ds(at, hd), :] = left


def attn_bwd(info, mine, got, out_keep, out_send, grad_keep, grad_send, lse, hd):
    cols, tok = mine.shape
    heads_k = cols // (4 * hd)
    width = tok // 2
    keep = pl.BlockSpec((width, 2 * hd), lambda h, i, info: (keep_block(i, info), h))
    send = pl.BlockSpec((width, 2 * hd), lambda h, i, info: (send_block(i, info), h))
    full = pl.BlockSpec((cols, tok), lambda h, i, info: (0, 0))
    return pl.pallas_call(
        functools.partial(attn_bwd_kernel, width, hd),
        grid_spec=pltpu.PrefetchScalarGridSpec(
            num_scalar_prefetch=1,
            grid=(heads_k, 4),
            in_specs=[
                ANY,
                ANY,
                keep,
                send,
                keep,
                send,
                pl.BlockSpec((1, 2, width), lambda h, i, info: (h, 0, i)),
            ],
            out_specs=[full, full],
            scratch_shapes=[
                pltpu.VMEM((cols, 2 * tok), BF16),
                pltpu.VMEM((2 * tok, 2 * hd), BF16),
                pltpu.VMEM((2 * tok, hd), BF16),
                pltpu.VMEM((2 * tok, hd), F32),
                pltpu.VMEM((2 * tok, hd), F32),
                pltpu.SemaphoreType.DMA((2,)),
            ],
        ),
        out_shape=[shape_of((cols, tok), BF16), shape_of((cols, tok), BF16)],
        compiler_params=settings(2, 60),
        cost_estimate=cost(True, 16.2),
        name="attn_bwd",
    )(info, mine, got, out_keep, out_send, grad_keep, grad_send, lse)


def load_blocks(plan, pieces, target, sem):
    rows = target.shape[1] // 4

    @pl.when(pl.program_id(0) == 0)
    def _():
        for k, places in enumerate(plan):
            for p, (piece, row) in enumerate(places):
                src = pieces[piece].at[pl.ds(row, rows)]
                pltpu.make_async_copy(src, target.at[k, pl.ds(p * rows, rows)], sem).start()
        pltpu.make_async_copy(target, target, sem).wait()


def out_proj_kernel(plan, count, info, *refs):
    x_ref, a0, a1, b0, b1, gain_ref, r_ref, n_ref, nt_ref, att_ref, w_ref, sem = refs[count:]
    load_blocks(plan, refs, w_ref, sem)
    ctx = info[2]
    total = x_ref[...].astype(F32)
    for j, ref, side in ((0, a0, ctx), (1, a1, ctx), (0, b0, 1 - ctx), (1, b1, 1 - ctx)):
        block = 2 * side + j
        part = ref[...]
        att_ref[block] = part
        total = total + dot(part, w_ref[block], 1, 1)
    rho = lax.rsqrt(jnp.mean(total * total, axis=-1, keepdims=True) + EPS)
    normed = total * rho * gain_ref[...]
    r_ref[...] = total
    n_ref[...] = normed.astype(BF16)
    nt_ref[...] = normed.T.astype(BF16)


def out_proj(info, x, mine, theirs, weights, gain, tile):
    plan, pieces = weights
    tok, width = x.shape
    feats = pieces[0].shape[1]
    rows_of = lambda n: pl.BlockSpec((tile, n), lambda i, info: (i, 0))
    return pl.pallas_call(
        functools.partial(out_proj_kernel, plan, len(pieces)),
        grid_spec=pltpu.PrefetchScalarGridSpec(
            num_scalar_prefetch=1,
            grid=(tok // tile,),
            in_specs=[ANY] * len(pieces)
            + [rows_of(width)]
            + [rows_of(feats)] * 4
            + [pl.BlockSpec((1, width), lambda i, info: (0, 0))],
            out_specs=[
                rows_of(width),
                rows_of(width),
                pl.BlockSpec((width, tile), lambda i, info: (0, i)),
                pl.BlockSpec((4, tile, feats), lambda i, info: (0, i, 0)),
            ],
            scratch_shapes=[pltpu.VMEM((4, width, feats), BF16), pltpu.SemaphoreType.DMA],
        ),
        out_shape=[
            shape_of((tok, width), F32),
            shape_of((tok, width), BF16),
            shape_of((width, tok), BF16),
            shape_of((4, tok, feats), BF16),
        ],
        compiler_params=settings(1, 60),
        cost_estimate=cost(True),
        name="out_proj",
    )(info, *pieces, x, *mine, *theirs, gain)


def norm_two_back_kernel(plan, count, info, *refs):
    g_ref, r_ref, gr_ref, gain_ref, gres_ref, gat_ref, a0, a1, b0, b1, gg_ref, w_ref, sem = refs[count:]
    load_blocks(plan, refs, w_ref, sem)
    ctx = info[2]
    grad, resid = g_ref[...], r_ref[...]
    rho = lax.rsqrt(jnp.mean(resid * resid, axis=-1, keepdims=True) + EPS)
    unit = resid * rho
    scaled = grad * gain_ref[...]
    back = rho * (scaled - unit * jnp.mean(scaled * unit, axis=-1, keepdims=True))
    total = gr_ref[...] + back
    gres_ref[...] = total
    low = total.astype(BF16)
    gat_ref[...] = total.T.astype(BF16)

    @pl.when(pl.program_id(0) == 0)
    def _():
        gg_ref[...] = jnp.zeros_like(gg_ref)

    gg_ref[...] += jnp.sum(grad * unit, axis=0, keepdims=True)
    for j, ref, side in ((0, a0, ctx), (1, a1, ctx), (0, b0, 1 - ctx), (1, b1, 1 - ctx)):
        ref[...] = dot(low, w_ref[2 * side + j], 1, 0).astype(BF16)


def norm_two_back(info, grad, resid, grad_result, gain, weights, tile):
    plan, pieces = weights
    tok, width = grad.shape
    feats = pieces[0].shape[1]
    rows_of = lambda n: pl.BlockSpec((tile, n), lambda i, info: (i, 0))
    row = pl.BlockSpec((1, width), lambda i, info: (0, 0))
    return pl.pallas_call(
        functools.partial(norm_two_back_kernel, plan, len(pieces)),
        grid_spec=pltpu.PrefetchScalarGridSpec(
            num_scalar_prefetch=1,
            grid=(tok // tile,),
            in_specs=[ANY] * len(pieces) + [rows_of(width)] * 3 + [row],
            out_specs=[rows_of(width), pl.BlockSpec((width, tile), lambda i, info: (0, i))]
            + [rows_of(feats)] * 4
            + [row],
            scratch_shapes=[pltpu.VMEM((4, width, feats), BF16), pltpu.SemaphoreType.DMA],
        ),
        out_shape=[shape_of((tok, width), F32), shape_of((width, tok), BF16)]
        + [shape_of((tok, feats), BF16)] * 4
        + [shape_of((1, width), F32)],
        compiler_params=settings(1, 60),
        cost_estimate=cost(True, 5.4),
        name="norm_two_back",
    )(info, *pieces, grad, resid, grad_result, gain)


def norm_one_back_kernel(plan, count, info, *refs):
    p0, p1, x_ref, gres_ref, gain_ref, out_ref, gg_ref, w_ref, sem = refs[count:]
    load_blocks(plan, refs, w_ref, sem)
    quarter = x_ref.shape[1] // 4
    grad = dot(p0[0], w_ref[0], 1, 1)
    grad = grad + dot(p1[0], w_ref[1], 1, 1)
    grad = grad + dot(p0[1], w_ref[2], 1, 1)
    grad = grad + dot(p1[1], w_ref[3], 1, 1)
    x = x_ref[...].astype(F32)
    rho = lax.rsqrt(jnp.mean(x * x, axis=-1, keepdims=True) + EPS)
    unit = x * rho
    scaled = grad * gain_ref[...]
    back = rho * (scaled - unit * jnp.mean(scaled * unit, axis=-1, keepdims=True))
    total = (gres_ref[...] + back).astype(BF16)
    for p, mask in enumerate(MASKS):
        at = pl.multiple_of(jnp.bitwise_xor(info[1], mask) * quarter, quarter)
        part = total[:, p * quarter : (p + 1) * quarter]

        out_ref[:, pl.ds(at, quarter)] = part

    @pl.when(pl.program_id(0) == 0)
    def _():
        gg_ref[...] = jnp.zeros_like(gg_ref)

    gg_ref[...] += jnp.sum(grad * unit, axis=0, keepdims=True)


def norm_one_back(info, pairs, weights, x, grad_resid, gain, tile, part):
    plan, pieces = weights
    tok, width = x.shape
    cols = pieces[0].shape[1]
    steps = tok // tile // 2
    first = part * steps
    rows_of = lambda n: pl.BlockSpec((tile, n), lambda i, info: (first + i, 0))
    out_rows = pl.BlockSpec((tile, width), lambda i, info: (i, 0))
    pair = pl.BlockSpec((2, tile, cols), lambda i, info: (0, first + i, 0))
    row = pl.BlockSpec((1, width), lambda i, info: (0, 0))
    return pl.pallas_call(
        functools.partial(norm_one_back_kernel, plan, len(pieces)),
        grid_spec=pltpu.PrefetchScalarGridSpec(
            num_scalar_prefetch=1,
            grid=(steps,),
            in_specs=[ANY] * len(pieces) + [pair, pair, rows_of(width), rows_of(width), row],
            out_specs=[out_rows, row],
            scratch_shapes=[pltpu.VMEM((4, width, cols), BF16), pltpu.SemaphoreType.DMA],
        ),
        out_shape=[shape_of((tok // 2, width), BF16), shape_of((1, width), F32)],
        compiler_params=settings(1, 60),
        cost_estimate=cost(True),
        name="norm_one_back",
    )(info, *pieces, *pairs, x, grad_resid, gain)


def weight_copies(plan, pieces, gate_up, down, gate_up_sem, down_sem):
    third = down.shape[1] // 3
    rows = down.shape[0] // 4
    wide, thin = [], []
    for p, chunks in enumerate(plan):
        block = pl.ds(p * rows, rows)
        for j, (piece, row, at) in enumerate(chunks):
            src = pieces[piece].at[pl.ds(row, rows)]
            wide.append(
                pltpu.make_async_copy(
                    src.at[:, pl.ds(at, 2 * third)],
                    gate_up.at[block, pl.ds(j * 2 * third, 2 * third)],
                    gate_up_sem,
                )
            )
            thin.append(
                pltpu.make_async_copy(
                    src.at[:, pl.ds(at + 2 * third, third)],
                    down.at[block, pl.ds(j * third, third)],
                    down_sem,
                )
            )
    return wide, thin


def split_act(act):
    third = act.shape[1] // 6
    part = lambda j: act[:, j * third : (j + 1) * third]
    return [(part(0), part(1)), (part(2), part(3)), (part(4), part(5))]


def ffn_fwd_kernel(tile, plans, last, info, scale, x_ref, in_ref, *rest):
    if last:
        teach_ref, rest = rest[0], rest[1:]
    pieces = []
    for plan in plans:
        count = 1 + max(place[0] for chunks in plan for place in chunks)
        pieces.append(rest[:count])
        rest = rest[count:]
    act_ref, hid_ref = rest[:2]
    if last:
        out_ref, gres_ref, low_ref, lowt_ref, sq_ref = rest[2:7]
        gate_up, down, total, sems = rest[7:]
    else:
        sum_ref, gate_up, down, total, sems = rest[2:]
    step, part = pl.program_id(0), pl.program_id(1)
    final = len(plans) - 1
    width = x_ref.shape[1]
    quarter = width // 4
    third = down.shape[2] // 3

    def copies(s):
        return weight_copies(
            plans[s], pieces[s], gate_up.at[s], down.at[s], sems.at[s, 0], sems.at[s, 1]
        )

    @pl.when((step == 0) & (part == 0))
    def _():
        for s in range(len(plans)):
            wide, thin = copies(s)
            for copy in wide + thin:
                copy.start()

    for s in range(len(plans)):

        @pl.when((step == s) & (part == 0))
        def _():
            pltpu.make_async_copy(gate_up.at[s], gate_up.at[s], sems.at[s, 0]).wait()

    rows = pl.ds(pl.multiple_of(part * tile, tile), tile)
    act = dot(x_ref[rows, :], gate_up[step], 1, 0)
    for j, (gate, upper) in enumerate(split_act(act)):
        sig = sigmoid(gate)
        silu = gate * sig
        hid_ref[0, :, j * third : (j + 1) * third] = (silu * upper).astype(BF16)
        at = 2 * j * third
        act_ref[0, :, at : at + third] = (upper * (sig + silu - silu * sig)).astype(BF16)
        act_ref[0, :, at + third : at + 2 * third] = silu.astype(BF16)
    for s in range(len(plans)):

        @pl.when((step == s) & (part == 0))
        def _():
            pltpu.make_async_copy(down.at[s], down.at[s], sems.at[s, 1]).wait()

    grown = dot(hid_ref[0], down[step], 1, 1)

    @pl.when(step == 0)
    def _():
        total[rows, :] = in_ref[...] + grown

    @pl.when(step > 0)
    def _():
        total[rows, :] += grown

    @pl.when(step == final)
    def _():
        result = total[rows, :]
        if not last:
            sum_ref[...] = result
            return
        tok = x_ref.shape[0]
        slot = info[2] * tok + part * tile + lax.broadcasted_iota(jnp.int32, (tile, 1), 0)
        valid = jnp.where(slot < info[3], 1.0, 0.0)
        square = jnp.zeros((tile, quarter), F32)
        for p, mask in enumerate(MASKS):
            at = pl.multiple_of(jnp.bitwise_xor(info[1], mask) * quarter, quarter)
            cols = slice(p * quarter, (p + 1) * quarter)
            value = result[:, cols]
            out_ref[:, pl.ds(at, quarter)] = value.astype(BF16)
            error = valid * (value - teach_ref[0, :, pl.ds(at, quarter)].astype(F32))
            square = square + error * error
            grad = error * scale[0]
            gres_ref[:, cols] = grad
            low_ref[:, cols] = grad.astype(BF16)
            lowt_ref[cols, :] = grad.T.astype(BF16)

        @pl.when(part == 0)
        def _():
            sq_ref[...] = jnp.zeros_like(sq_ref)

        sq_ref[...] += jnp.sum(square, axis=0, keepdims=True)


def ffn_fwd(info, scale, x, total, teacher, weights, units, tile):
    tok, width = x.shape
    pieces = [piece for _, group in weights for piece in group]
    count = len(weights)
    last = teacher is not None
    entry = lambda s, i: jnp.where(s == 0, i, tok // tile - 1)
    leave = lambda s, i: jnp.where(s == count - 1, i, 0)
    tiles = lambda n: pl.BlockSpec((tile, n), lambda s, i, info: (leave(s, i), 0))
    slab = lambda n: pl.BlockSpec((1, tile, n), lambda s, i, info: (s, i, 0))
    in_specs = [
        SMEM,
        whole((tok, width)),
        pl.BlockSpec((tile, width), lambda s, i, info: (entry(s, i), 0)),
    ]
    out_specs = [slab(2 * units), slab(units)]
    out_shape = [shape_of((count, tok, 2 * units), BF16), shape_of((count, tok, units), BF16)]
    if last:
        in_specs.append(
            pl.BlockSpec((1, tile, width), lambda s, i, info: (info[0], leave(s, i), 0))
        )
        out_specs += [
            tiles(width),
            tiles(width),
            tiles(width),
            pl.BlockSpec((width, tile), lambda s, i, info: (0, leave(s, i))),
            pl.BlockSpec((1, width // 4), lambda s, i, info: (0, 0)),
        ]
        out_shape += [
            shape_of((tok, width), BF16),
            shape_of((tok, width), F32),
            shape_of((tok, width), BF16),
            shape_of((width, tok), BF16),
            shape_of((1, width // 4), F32),
        ]
    else:
        out_specs.append(tiles(width))
        out_shape.append(shape_of((tok, width), F32))
    return pl.pallas_call(
        functools.partial(ffn_fwd_kernel, tile, [plan for plan, _ in weights], last),
        grid_spec=pltpu.PrefetchScalarGridSpec(
            num_scalar_prefetch=1,
            grid=(count, tok // tile),
            in_specs=in_specs + [ANY] * len(pieces),
            out_specs=out_specs,
            scratch_shapes=[
                pltpu.VMEM((count, width, 2 * units), BF16),
                pltpu.VMEM((count, width, units), BF16),
                pltpu.VMEM((tok, width), F32),
                pltpu.SemaphoreType.DMA((count, 2)),
            ],
        ),
        out_shape=out_shape,
        compiler_params=settings(2, 60),
        cost_estimate=cost(True),
        name="ffn_fwd",
    )(info, scale, x, total, *([teacher] if last else []), *pieces)


def ffn_bwd_kernel(steps, plan, first, low_ref, act_ref, hid_ref, xt_ref, lowt_ref, *rest):
    count = 1 + max(place[0] for chunks in plan for place in chunks)
    pieces, rest = rest[:count], rest[count:]
    if not first:
        in_ref, rest = rest[0], rest[1:]
    out_ref, keep_ref, send_ref, gate_up, down, dact_all, hid_all, sems = rest
    step = pl.program_id(0)
    units = down.shape[1]
    third = units // 3
    tile = low_ref.shape[0]

    @pl.when(step == 0)
    def _():
        wide, thin = weight_copies(plan, pieces, gate_up, down, sems.at[0], sems.at[1])
        for copy in thin + wide:
            copy.start()
        pltpu.make_async_copy(down, down, sems.at[1]).wait()

    @pl.when(step < steps)
    def _():
        rows = pl.ds(pl.multiple_of(step * tile, tile), tile)
        grad_hidden = dot(low_ref[...], down[...], 1, 0)
        for j, (to_gate, to_upper) in enumerate(split_act(act_ref[0])):
            grad = grad_hidden[:, j * third : (j + 1) * third]
            at = 2 * j * third
            dact_all[rows, at : at + third] = (grad * to_gate.astype(F32)).astype(BF16)
            dact_all[rows, at + third : at + 2 * third] = (grad * to_upper.astype(F32)).astype(BF16)
        hid_all[rows, :] = hid_ref[0]

        @pl.when(step == 0)
        def _():
            pltpu.make_async_copy(gate_up, gate_up, sems.at[0]).wait()

        grown = dot(dact_all[rows, :], gate_up[...], 1, 1)
        out_ref[...] = grown if first else in_ref[...] + grown

    def weight_rows(target):
        target[:, : 2 * units] = dot(xt_ref[...], dact_all[...], 1, 0).astype(BF16)
        target[:, 2 * units :] = dot(lowt_ref[...], hid_all[...], 1, 0).astype(BF16)

    @pl.when((step >= steps) & (step < steps + 2))
    def _():
        weight_rows(send_ref)

    @pl.when(step >= steps + 2)
    def _():
        weight_rows(keep_ref)


def ffn_bwd(low, saved, weights, total, xt, lowt, tile):
    plan, pieces = weights
    acts, hiddens, block = saved
    tok, width = low.shape
    units = hiddens.shape[2]
    steps = tok // tile
    quarter = width // 4
    first = total is None
    clip = lambda i: jnp.minimum(i, steps - 1)
    rows_of = lambda n: pl.BlockSpec((tile, n), lambda i: (clip(i), 0))
    slab = lambda n: pl.BlockSpec((1, tile, n), lambda i: (block, clip(i), 0))
    feature = lambda i: (jnp.where(i < steps + 2, jnp.maximum(i - steps, 0) + 2, i - steps - 2), 0)
    return pl.pallas_call(
        functools.partial(ffn_bwd_kernel, steps, plan, first),
        grid=(steps + 4,),
        in_specs=[
            rows_of(width),
            slab(2 * units),
            slab(units),
            pl.BlockSpec((quarter, tok), feature),
            pl.BlockSpec((quarter, tok), feature),
        ]
        + [ANY] * len(pieces)
        + ([] if first else [rows_of(width)]),
        out_specs=[
            rows_of(width),
            pl.BlockSpec((quarter, 3 * units), lambda i: (jnp.maximum(i - steps - 2, 0), 0)),
            pl.BlockSpec((quarter, 3 * units), lambda i: (jnp.clip(i - steps, 0, 1), 0)),
        ],
        out_shape=[
            shape_of((tok, width), F32),
            shape_of((width // 2, 3 * units), BF16),
            shape_of((width // 2, 3 * units), BF16),
        ],
        scratch_shapes=[
            pltpu.VMEM((width, 2 * units), BF16),
            pltpu.VMEM((width, units), BF16),
            pltpu.VMEM((tok, 2 * units), BF16),
            pltpu.VMEM((tok, units), BF16),
            pltpu.SemaphoreType.DMA((2,)),
        ],
        input_output_aliases={} if first else {5 + len(pieces): 0},
        compiler_params=settings(1, 60),
        cost_estimate=cost(True, 11.2),
        name="ffn_bwd",
    )(low, acts, hiddens, xt, lowt, *pieces, *([] if first else [total]))


def turn_chunks(block):
    wide = block.shape[1] * 2 // 9
    thin = wide // 2
    starts = [(2 * wide, wide), (wide, wide), (0, wide)]
    starts += [(3 * wide + 2 * thin, thin), (3 * wide + thin, thin), (3 * wide, thin)]
    return jnp.concatenate([block[:, a : a + n] for a, n in starts], axis=1)


def sum_kernel(turns, *refs):
    total = None
    for ref, turn in zip(refs[:-1], turns):
        value = ref[...].astype(F32)
        value = turn_chunks(value) if turn else value
        total = value if total is None else total + value
    refs[-1][...] = total.astype(refs[-1].dtype)


def summed(terms, turns=None, dtype=BF16):
    rows, cols = terms[0].shape
    spec = pl.BlockSpec((128, cols), lambda i: (i, 0))
    return pl.pallas_call(
        functools.partial(sum_kernel, turns or [False] * len(terms)),
        grid=(rows // 128,),
        in_specs=[spec] * len(terms),
        out_specs=spec,
        out_shape=shape_of((rows, cols), dtype),
        compiler_params=settings(1, 60),
        cost_estimate=cost(False),
        name="summed",
    )(*terms)


def sums_kernel(jobs, count, info, *refs):
    arrays, refs = refs[:count], refs[count:]
    outs, (term_buf, out_buf, term_sems, out_sems) = refs[: len(jobs)], refs[len(jobs) :]
    rows = term_buf.shape[1]
    copies = []
    for terms in jobs:
        group = []
        for array, base, pick, _ in terms:
            at = base
            if pick is not None:
                at = pl.multiple_of(base + jnp.bitwise_xor(info[2], pick) * rows, rows)
            i = len(copies) + len(group)
            src = arrays[array].at[pl.ds(at, rows)]
            group.append(pltpu.make_async_copy(src, term_buf.at[i], term_sems.at[i]))
            group[-1].start()
        copies += group
    first = 0
    stores = []
    for j, terms in enumerate(jobs):
        total = None
        for i, (_, _, _, turn) in enumerate(terms):
            copies[first + i].wait()
            value = term_buf[first + i].astype(F32)
            value = turn_chunks(value) if turn else value
            total = value if total is None else total + value
        first += len(terms)
        out_buf[j] = total.astype(BF16)
        stores.append(pltpu.make_async_copy(out_buf.at[j], outs[j], out_sems.at[j]))
        stores[-1].start()
    for store in stores:
        store.wait()


def sums(info, arrays, jobs):
    cols = arrays[0].shape[1]
    rows, terms = 128, sum(len(job) for job in jobs)
    return pl.pallas_call(
        functools.partial(sums_kernel, jobs, len(arrays)),
        grid_spec=pltpu.PrefetchScalarGridSpec(
            num_scalar_prefetch=1,
            grid=(1,),
            in_specs=[ANY] * len(arrays),
            out_specs=[ANY] * len(jobs),
            scratch_shapes=[
                pltpu.VMEM((terms, rows, cols), BF16),
                pltpu.VMEM((len(jobs), rows, cols), BF16),
                pltpu.SemaphoreType.DMA((terms,)),
                pltpu.SemaphoreType.DMA((len(jobs),)),
            ],
        ),
        out_shape=[shape_of((rows, cols), BF16)] * len(jobs),
        compiler_params=settings(1, 60),
        cost_estimate=cost(False),
        name="sums",
    )(info, *arrays)


def core_jobs(keep, came):
    return [[(a, far * 256, pick, False) for a in (keep, came)] for far in (0, 1) for pick in (0, 1)]


def core_sum_kernel(info, left_ref, right_ref, *outs):
    total = (left_ref[...].astype(F32) + right_ref[...].astype(F32)).astype(BF16)
    block = pl.program_id(1)
    place = block // 2 * 2 + jnp.bitwise_xor(block % 2, info[2])
    for i, out in enumerate(outs):

        @pl.when(place == i)
        def _():
            out[...] = total


def core_sum(info, keep, came):
    groups, rows, cols = keep.shape
    spec = pl.BlockSpec((1, rows // 4, cols), lambda g, i, info: (g, i, 0))
    return pl.pallas_call(
        core_sum_kernel,
        grid_spec=pltpu.PrefetchScalarGridSpec(
            num_scalar_prefetch=1,
            grid=(groups, 4),
            in_specs=[spec] * 2,
            out_specs=[pl.BlockSpec((1, rows // 4, cols), lambda g, i, info: (g, 0, 0))] * 4,
        ),
        out_shape=[shape_of((groups, rows // 4, cols), BF16)] * 4,
        compiler_params=settings(2, 24),
        cost_estimate=cost(False),
        name="core_sum",
    )(info, keep, came)


def weight_grad_kernel(nt_ref, back0_ref, back1_ref, gt_ref, att_ref, keep_ref, send_ref):
    cols = back0_ref.shape[2]
    part, block = pl.program_id(0), pl.program_id(1)

    def rows(target, back_ref):
        target[0, :, :cols] = dot(nt_ref[...], back_ref[0], 1, 0).astype(BF16)
        target[0, :, cols:] = dot(gt_ref[...], att_ref[0], 1, 0).astype(BF16)

    for j, back_ref in enumerate((back0_ref, back1_ref)):

        @pl.when((part == 0) & (block % 2 == j))
        def _():
            rows(send_ref, back_ref)

        @pl.when((part == 1) & (block % 2 == j))
        def _():
            rows(keep_ref, back_ref)


def weight_grad(normed_t, backs, grad_t, attended):
    width, tok = normed_t.shape
    cols, feats = backs[0].shape[2], attended.shape[2]
    half = pl.BlockSpec((width // 2, tok), lambda p, k: (1 - p, 0))
    side = pl.BlockSpec((1, tok, cols), lambda p, k: (k // 2, 0, 0))
    shape = (1, width // 2, cols + feats)
    return pl.pallas_call(
        weight_grad_kernel,
        grid=(2, 4),
        in_specs=[half, side, side, half, pl.BlockSpec((1, tok, feats), lambda p, k: (k, 0, 0))],
        out_specs=[
            pl.BlockSpec(shape, lambda p, k: (jnp.where(p == 0, 0, k), 0, 0)),
            pl.BlockSpec(shape, lambda p, k: (jnp.where(p == 0, k, 3), 0, 0)),
        ],
        out_shape=[shape_of((4, width // 2, cols + feats), BF16)] * 2,
        compiler_params=settings(2, 60),
        cost_estimate=cost(True),
        name="weight_grad",
    )(normed_t, *backs, grad_t, attended)


def copy_kernel(in_ref, out_ref):
    out_ref[...] = in_ref[...]


def copied(array):
    spec = pl.BlockSpec((1,) + array.shape[1:], lambda i: (i, 0, 0))
    return pl.pallas_call(
        copy_kernel,
        grid=(array.shape[0],),
        in_specs=[spec],
        out_specs=spec,
        out_shape=shape_of(array.shape, array.dtype),
        compiler_params=settings(1, 24),
        cost_estimate=cost(False),
        name="copied",
    )(array)


def after(value, *others):
    return lax.optimization_barrier((value,) + others)[0]


def per_device_rows(
    tokens,
    teacher,
    lengths,
    attn_gain,
    q_weight,
    k_weight,
    v_weight,
    q_gain,
    k_gain,
    o_weight,
    ffn_gain,
    gate_weight,
    up_weight,
    down_weight,
):
    z = lax.axis_index("tp")
    ctx = lax.axis_index("ctx")
    fsdp = lax.axis_index("fsdp")
    rows_dev, tok, width = tokens.shape
    quarter = width // 4
    hd = q_gain.shape[0] * 4
    q_cols, k_cols = q_weight.shape[1], k_weight.shape[1]
    proj = q_cols + 2 * k_cols
    heads = (q_cols // hd, k_cols // hd)
    units = gate_weight.shape[1]
    slots = rows_dev * 4 * tok * 2

    def x_swap(v):
        return lax.ppermute(v, "fsdp", X_SWAP)

    def core_swap(v):
        return lax.ppermute(v, "fsdp", CORE_SWAP)

    def y_swap(v):
        return lax.ppermute(v, "ctx", Y_SWAP)

    def z_up(v):
        return lax.ppermute(v, "tp", Z_UP)

    def z_far(v):
        return lax.ppermute(v, "tp", Z_FAR)

    def z_down(v):
        return lax.ppermute(v, "tp", Z_DOWN)

    def natural(v):
        v = jnp.concatenate([v[0:1], v[2:3], v[1:2], v[3:4]], axis=0)
        v = jnp.where(fsdp % 2 == 0, v, jnp.concatenate([v[1:2], v[0:1], v[3:4], v[2:3]], axis=0))
        return jnp.where(fsdp // 2 == 0, v, jnp.concatenate([v[2:4], v[0:2]], axis=0))

    v = {}

    def sync():
        v.update(lax.optimization_barrier(dict(v)))

    length = lax.dynamic_slice_in_dim(lengths, z, 1, 0)
    info = jnp.concatenate([jnp.stack([z, fsdp, ctx]).astype(jnp.int32), length])
    w_proj = join(q_weight, k_weight, v_weight)
    proj_z = [z_up(w_proj), z_far(w_proj), z_down(w_proj)]
    proj_own = jnp.concatenate([w_proj, x_swap(w_proj)], axis=0)
    count_here = jnp.sum(lengths).astype(F32)[None]
    vector = jnp.concatenate([attn_gain, ffn_gain, q_gain, k_gain]).astype(F32)
    vector = jnp.concatenate([vector, count_here, jnp.zeros((640 - 545,), F32)])[None]
    vector = jnp.concatenate([vector, x_swap(vector)], axis=0)
    vector = jnp.concatenate([vector, core_swap(vector)], axis=0)
    w_out, w_ffn, *w_chunks = pack(info, o_weight, gate_weight, up_weight, down_weight)
    pos = (ctx * tok + jnp.arange(tok, dtype=jnp.int32)).astype(F32)
    frequency = THETA ** (-(2.0 * jnp.arange(hd // 2, dtype=F32)) / hd)
    angles = frequency[:, None] * pos[None, :]
    head_gains = natural(vector[:, 2 * quarter : 544])
    v.update(
        info=info,
        proj_own=proj_own,
        proj_z=jnp.concatenate(proj_z, axis=0),
        w_out=w_out,
        w_ffn=w_ffn,
        w_chunks=w_chunks,
        gain_one=vector[:, :quarter].reshape(1, width),
        gain_two=vector[:, quarter : 2 * quarter].reshape(1, width),
        total_count=jnp.sum(vector[:, 544]),
        gain_q=head_gains[:, : hd // 4].reshape(hd, 1),
        gain_k=head_gains[:, hd // 4 :].reshape(hd, 1),
        cos_part=jnp.cos(angles),
        sin_part=jnp.sin(angles),
    )
    sync()
    info = v["info"]

    proj_zfar = x_swap(v["proj_z"])
    out_z = [z_up(v["w_out"]), z_far(v["w_out"]), z_down(v["w_out"])]
    own_core = core_swap(v["proj_own"])
    x_in, normed_one_t = norm_one(info, tokens, v["gain_one"], 256)
    v.update(
        proj_zfar=proj_zfar, own_core=own_core, x_in=x_in, normed_one_t=normed_one_t, out_z=out_z
    )
    sync()

    plan_proj = [[(0, 0), (0, quarter), (3, 0), (3, quarter)]]
    plan_proj += [[(p, k * quarter) for p in (1, 2, 4, 5)] for k in range(3)]
    weights_proj = [v["proj_own"], v["proj_z"], v["proj_zfar"], v["own_core"]]
    weights_proj += [core_swap(v["proj_z"]), core_swap(v["proj_zfar"])]
    one = [z_up(v["w_chunks"][0]), z_up(v["w_chunks"][3])]
    ffn_far = x_swap(v["w_ffn"])
    tables = [v[name] for name in ("cos_part", "sin_part", "gain_q", "gain_k")]

    def make(block, *then):
        normed_t = after(v["normed_one_t"], *then)
        return project(info, (plan_proj, weights_proj), normed_t, *tables, heads, block)

    theirs = [make(lambda s: 2 * (1 - s[2]))]
    got = [y_swap(theirs[0][0])]
    theirs.append(make(lambda s: 2 * (1 - s[2]) + 1, theirs[0][0]))
    got.append(y_swap(theirs[1][0]))
    mine = [make(lambda s: 2 * s[2], theirs[1][0])]
    mine.append(make(lambda s: 2 * s[2] + 1, mine[0][0]))
    v.update(
        one=one,
        ffn_far=ffn_far,
        weights_proj=weights_proj,
        mine=mine,
        theirs=theirs,
        got0=got[0],
    )
    sync()

    one_far = [x_swap(v["one"][0])]
    three = [z_down(v["w_chunks"][0])]
    own_cores = [core_swap(v["w_ffn"]), core_swap(v["ffn_far"])]
    first = attn_fwd(info, v["mine"][0][0], v["got0"], hd)
    v.update(first=first, got1=got[1], one_far=one_far, three=three, own_cores=own_cores)
    sync()

    arrived = [y_swap(v["first"][1])]
    three = v["three"] + [z_down(v["w_chunks"][1])]
    out_blocks = jnp.concatenate([v["w_out"]] + v["out_z"], axis=0)
    out_far = x_swap(out_blocks)
    one_cores = [core_swap(v["one"][0]), core_swap(v["one_far"][0])]
    second = attn_fwd(info, v["mine"][1][0], v["got1"], hd)
    v.update(
        second=second,
        arrived=arrived,
        three=three,
        out_blocks=out_blocks,
        out_far=out_far,
        one_cores=one_cores,
    )
    sync()

    arrived = v["arrived"] + [y_swap(v["second"][1])]
    three = v["three"] + [z_down(v["w_chunks"][2])]
    one_far = v["one_far"] + [x_swap(v["one"][1][:, :units])]
    weights_out = [v["out_blocks"], v["out_far"]]
    weights_out += [core_swap(v["out_blocks"]), core_swap(v["out_far"])]
    v.update(arrived=arrived, three=three, one_far=one_far, weights_out=weights_out)
    sync()

    plan_out = [[(p, k * quarter) for p in range(4)] for k in range(4)]
    two = [z_up(v["one"][0])]
    three_far = [x_swap(v["three"][0])]
    one_far = v["one_far"] + [y_swap(v["one_far"][0])]
    one_cores = v["one_cores"] + [core_swap(v["one"][1]), core_swap(v["one_far"][1])]
    resid, normed_two, normed_two_t, attended = out_proj(
        info,
        v["x_in"],
        [v["first"][0], v["second"][0]],
        v["arrived"],
        (plan_out, v["weights_out"]),
        v["gain_two"],
        256,
    )
    v.update(
        two=two,
        three_far=three_far,
        one_far=one_far,
        one_cores=one_cores,
        resid=resid,
        normed_two=normed_two,
        normed_two_t=normed_two_t,
        attended=attended,
    )
    sync()

    plan0 = [[(i, 0, j * units) for j in range(3)] for i in range(4)]
    plan_mixed = [[(0, 0, 0), (1, 0, 0), (1, 0, units)], [(i, 0, 0) for i in (2, 3, 4)]]
    plan_mixed += [[(5, 0, 0), (6, 0, 0), (6, 0, units)], [(i, 0, 0) for i in (7, 8, 9)]]
    scale = (slots / v["total_count"])[None]
    weights0 = [v["w_ffn"], v["ffn_far"]] + v["own_cores"]
    c0, cf, c1, cb = v["one_cores"]
    weights1 = v["one"] + v["one_far"] + [c0, c1, cf, cb, core_swap(v["one_far"][2])]
    two = v["two"] + [z_up(v["one"][1])]
    three_far = v["three_far"] + [x_swap(v["three"][1]), y_swap(v["three_far"][0])]
    two_far = [x_swap(v["two"][0])]
    three_cores = [core_swap(v["three"][0])]
    acts_a, hiddens_a, sum_a = ffn_fwd(
        info,
        scale,
        v["normed_two"],
        v["resid"],
        None,
        [(plan0, weights0), (plan_mixed, weights1)],
        units,
        256,
    )
    v.update(
        scale=scale,
        weights0=weights0,
        weights1=weights1,
        two=two,
        three_far=three_far,
        two_far=two_far,
        three_cores=three_cores,
        acts_a=acts_a,
        hiddens_a=hiddens_a,
        sum_a=sum_a,
    )
    sync()

    plan_chunks = [[(3 * p + j, 0, 0) for j in range(3)] for p in range(4)]
    weights3 = v["three"] + v["three_far"] + v["three_cores"]
    weights3 += [core_swap(part) for part in v["three"][1:]]
    weights3 += [core_swap(part) for part in v["three_far"]]
    two_far = v["two_far"] + [x_swap(v["two"][1][:, :units]), y_swap(v["two_far"][0])]
    two_cores = [core_swap(part) for part in v["two"] + v["two_far"]]
    acts_b, hiddens_b, sum_b = ffn_fwd(
        info, v["scale"], v["normed_two"], v["sum_a"], None, [(plan_chunks, weights3)], units, 256
    )
    v.update(
        weights3=weights3,
        two_far=two_far,
        two_cores=two_cores,
        acts_b=acts_b,
        hiddens_b=hiddens_b,
        sum_b=sum_b,
    )
    sync()

    weights2 = v["two"] + v["two_far"] + v["two_cores"]
    weights2 += [core_swap(part) for part in v["two_far"][1:]]
    acts_c, hiddens_c, result_low, grad_result, grad_low, grad_low_t, square = ffn_fwd(
        info, v["scale"], v["normed_two"], v["sum_b"], teacher, [(plan_mixed, weights2)], units, 256
    )
    v.update(
        weights2=weights2,
        acts_c=acts_c,
        hiddens_c=hiddens_c,
        result_low=result_low,
        grad_result=grad_result,
        grad_low=grad_low,
        grad_low_t=grad_low_t,
        square=square,
    )
    sync()

    def ffn_back(plan, weights, acts, hiddens, block, total):
        return ffn_bwd(
            v["grad_low"],
            (v[acts], v[hiddens], block),
            (plan, v[weights]),
            total,
            v["normed_two_t"],
            v["grad_low_t"],
            256,
        )

    turned = [False, False, True]
    output = lax.all_gather(v["result_low"], "tp", axis=0, tiled=False)
    total, keep2, send2 = ffn_back(plan_mixed, "weights2", "acts_c", "hiddens_c", 0, None)
    v.update(total=total, keep2=keep2, send2=send2)
    sync()

    came2 = core_swap(v["send2"])
    total, keep1, send1 = ffn_back(plan_mixed, "weights1", "acts_a", "hiddens_a", 1, v["total"])
    v.update(came2=came2, total=total, keep1=keep1, send1=send1)
    sync()

    came1 = core_swap(v["send1"])
    sum2 = sums(info, [v["keep2"], v["came2"]], core_jobs(0, 1))
    far_t2 = x_swap(sum2[3])
    total, keep3, send3 = ffn_back(
        plan_chunks, "weights3", "acts_b", "hiddens_b", 0, after(v["total"], sum2[0])
    )
    v.update(
        came1=came1,
        sum2=sum2,
        far_t2=far_t2,
        total=total,
        keep3=keep3,
        send3=send3,
    )
    sync()

    came3 = core_swap(v["send3"])
    far_h2 = x_swap(v["sum2"][2])
    there2, *sum1 = sums(
        info,
        [v["sum2"][1], v["far_t2"], v["keep1"], v["came1"]],
        [[(0, 0, None, False), (1, 0, None, False)]] + core_jobs(2, 3),
    )
    there2 = y_swap(there2)
    total, keep0, send0 = ffn_back(
        plan0, "weights0", "acts_a", "hiddens_a", 0, after(v["total"], sum1[0])
    )
    v.update(
        came3=came3,
        far_h2=far_h2,
        there2=there2,
        sum1=sum1,
        total=total,
        keep0=keep0,
        send0=send0,
    )
    sync()

    came0 = core_swap(v["send0"])
    far_t1 = x_swap(v["sum1"][3])
    plane = [(0, 0, None, False), (1, 0, None, False), (2, 0, None, True)]
    part2, *sum3 = sums(
        info,
        [v["sum2"][0], v["far_h2"], v["there2"], v["keep3"], v["came3"]],
        [plane] + core_jobs(3, 4),
    )
    down2 = z_down(part2)
    grad_resid, grad_attn_t, a0, a1, b0, b1, gain_two_sum = norm_two_back(
        info,
        after(v["total"], sum3[0]),
        v["resid"],
        v["grad_result"],
        v["gain_two"],
        (plan_out, v["weights_out"]),
        256,
    )
    grad_got = [y_swap(b0), y_swap(b1)]
    v.update(
        came0=came0,
        far_t1=far_t1,
        sum3=sum3,
        grad_resid=grad_resid,
        grad_attn_t=grad_attn_t,
        grad_mine=[a0, a1],
        gain_two_sum=gain_two_sum,
        grad_got0=grad_got[0],
    )
    sync()

    def attn_back(j, grad):
        out, got_ref = v["first" if j == 0 else "second"], v[f"got{j}"]
        return attn_bwd(
            info, v["mine"][j][0], got_ref, out[0], out[1], grad, v[f"grad_got{j}"], out[2], hd
        )

    far_h1 = x_swap(v["sum1"][2])
    there1, *sum0 = sums(
        info,
        [v["sum1"][1], v["far_t1"], v["keep0"], v["came0"]],
        [[(0, 0, None, False), (1, 0, None, False)]] + core_jobs(2, 3),
    )
    there1 = y_swap(there1)
    far_t3 = x_swap(v["sum3"][3])
    back0 = attn_back(0, after(v["grad_mine"][0], sum0[0]))
    v.update(
        far_h1=far_h1,
        there1=there1,
        far_t3=far_t3,
        down2=down2,
        sum0=sum0,
        back0=back0,
        grad_got1=grad_got[1],
    )
    sync()

    heads0 = y_swap(v["back0"][1])
    far_h3 = x_swap(v["sum3"][2])
    far_t0 = x_swap(v["sum0"][3])
    there3, two_down = sums(
        info,
        [v["sum3"][1], v["far_t3"], v["sum1"][0], v["far_h1"], v["there1"], v["down2"]],
        [
            [(0, 0, None, False), (1, 0, None, False)],
            [(2, 0, None, False), (3, 0, None, False), (4, 0, None, True), (5, 0, None, False)],
        ],
    )
    there3_got = y_swap(there3)
    two_down_got = z_down(two_down)
    back1 = attn_back(1, after(v["grad_mine"][1], there3, two_down, output))
    v.update(
        heads0=heads0, far_h3=far_h3, far_t0=far_t0, there3=there3_got, back1=back1
    )
    sync()

    heads1 = y_swap(v["back1"][1])
    far_h0 = x_swap(v["sum0"][2])
    part3, there0 = sums(
        info,
        [v["sum3"][0], v["far_h3"], v["there3"], v["sum0"][1], v["far_t0"]],
        [plane, [(3, 0, None, False), (4, 0, None, False)]],
    )
    up3 = z_up(part3)
    tables = [v[name] for name in ("cos_part", "sin_part", "gain_q", "gain_k")]
    head0 = head_back(
        info, v["back0"][0], v["heads0"], v["mine"][0][1], v["theirs"][0][1], *tables, heads
    )
    v.update(heads1=heads1, head0=head0, there0=there0)
    sync()

    there0 = y_swap(v["there0"])
    head1 = head_back(
        info, v["back1"][0], v["heads1"], v["mine"][1][1], v["theirs"][1][1], *tables, heads
    )
    def last_norm(part, *then):
        return norm_one_back(
            info,
            [v["head0"][0], after(head1[0], *then)],
            (plan_proj, v["weights_proj"]),
            v["x_in"],
            v["grad_resid"],
            v["gain_one"],
            tok // 4,
            part,
        )

    low_first, gain_first = last_norm(0)
    low_second, gain_second = last_norm(1, low_first)
    gathered = [lax.all_gather(low_first, "tp", axis=0, tiled=False)]
    tokens_low, gain_one_sum = low_second, gain_first + gain_second
    v.update(head1=head1, tokens_low=tokens_low, gain_one_sum=gain_one_sum, up3=up3)
    v.update(there0=there0, far_h0=far_h0, two_down=two_down_got)
    sync()

    gathered.append(lax.all_gather(v["tokens_low"], "tp", axis=0, tiled=False))
    keep, send = weight_grad(
        v["normed_one_t"], [v["head0"][0], v["head1"][0]], v["grad_attn_t"], v["attended"]
    )
    gain_heads = v["head0"][1] + v["head1"][1]
    vector = jnp.concatenate(
        [
            natural(v["gain_one_sum"].reshape(4, quarter)).reshape(1, width),
            natural(v["gain_two_sum"].reshape(4, quarter)).reshape(1, width),
            gain_heads[:, 0].reshape(1, hd),
            gain_heads[:, 1].reshape(1, hd),
            jnp.sum(v["square"]).reshape(1, 1),
            jnp.zeros((1, 127), F32),
        ],
        axis=1,
    )
    vector = vector + core_swap(vector)
    v.update(keep=keep, send=send)
    v.update(vector=vector)
    sync()

    rows = quarter // 2
    flat = lambda a: a.reshape(4 * rows, a.shape[-1])
    attn_sums = [flat(p) for p in core_sum(info, v["keep"], core_swap(v["send"]))]
    vector = v["vector"] + x_swap(v["vector"])
    v.update(sums=attn_sums, vector=vector)
    sync()

    far_t = x_swap(v["sums"][3])
    part0 = summed([v["sum0"][0], v["far_h0"], v["there0"]], turned)
    ffn_sum = summed([part0, v["two_down"], v["up3"]], None, F32)
    vector = v["vector"] + y_swap(v["vector"])
    v.update(far_t=far_t, ffn_sum=ffn_sum, vector=vector)
    sync()

    far_h = x_swap(v["sums"][2])
    there = y_swap(summed([v["sums"][1], v["far_t"]]))
    spread = copied(output)
    v.update(far_h=far_h, there=there, spread=spread)
    sync()

    parts = summed([v["sums"][0], v["far_h"], v["there"]])
    parts = [parts[k * rows : (k + 1) * rows] for k in range(4)]
    parts = [parts[0], z_down(parts[1]), z_far(parts[2]), z_up(parts[3])]
    ffn_other = y_swap(v["ffn_sum"])
    v.update(parts=parts)
    sync()

    attn_sum = summed(v["parts"], None, F32)
    vector = v["vector"] + lax.ppermute(v["vector"], "tp", Z_NEAR)
    v.update(attn_sum=attn_sum, vector=vector)
    v.update(ffn_other=ffn_other)
    sync()

    def finish(own, other):
        return jnp.concatenate(
            [jnp.where(ctx == 0, own, other), jnp.where(ctx == 0, other, own)], axis=0
        )

    def columns(first):
        parts = [ffn_grad[:, first(j) : first(j) + third] for j in range(3)]
        return jnp.concatenate(
            [
                jnp.where(ctx == 0, parts[0], parts[2]),
                parts[1],
                jnp.where(ctx == 0, parts[2], parts[0]),
            ],
            axis=1,
        )

    attn_other = y_swap(v["attn_sum"])
    vector = v["vector"] + lax.ppermute(v["vector"], "tp", Z_FAR)
    third = units // 3
    ffn_grad = finish(v["ffn_sum"], turn_chunks(v["ffn_other"]))
    grad_gate = columns(lambda j: 2 * j * third)
    grad_up = columns(lambda j: (2 * j + 1) * third)
    grad_down = columns(lambda j: 2 * units + j * third).T
    grad = jnp.zeros((rows_dev, tok, width), F32)
    grad = lax.dynamic_update_slice(grad, gathered[0].astype(F32), (0, 0, 0))
    v.update(vector=vector, attn_other=attn_other, grad=grad)
    v.update(grad_gate=grad_gate, grad_up=grad_up, grad_down=grad_down)
    sync()

    tokens_grad = lax.dynamic_update_slice(v["grad"], gathered[1].astype(F32), (0, tok // 2, 0))
    sums_all = v["vector"][0]

    attn_grad = finish(v["attn_sum"], v["attn_other"])
    teacher_loss = sums_all[2 * width + 2 * hd] / (v["total_count"] * width)

    def own_part(at, size):
        return lax.dynamic_slice_in_dim(sums_all, at + fsdp * (size // 4), size // 4, 0)

    return (
        v["spread"],
        teacher_loss,
        tokens_grad,
        own_part(0, width),
        attn_grad[:, :q_cols],
        attn_grad[:, q_cols : q_cols + k_cols],
        attn_grad[:, q_cols + k_cols : proj],
        own_part(2 * width, hd),
        own_part(2 * width + hd, hd),
        attn_grad[:, proj:].T,
        own_part(width, width),
        v["grad_gate"],
        v["grad_up"],
        v["grad_down"],
    )


def solution(mesh):
    return jax.shard_map(
        per_device_rows if fits(mesh) else per_device_any,
        mesh=mesh,
        in_specs=(
            P("fsdp", "ctx", None),
            P("fsdp", "ctx", None),
            P("fsdp"),
            P("fsdp"),
            P("fsdp", "tp"),
            P("fsdp", "tp"),
            P("fsdp", "tp"),
            P("fsdp"),
            P("fsdp"),
            P("tp", "fsdp"),
            P("fsdp"),
            P("fsdp", "tp"),
            P("fsdp", "tp"),
            P("tp", "fsdp"),
        ),
        out_specs=(
            P("fsdp", "ctx", None),
            P(),
            P("fsdp", "ctx", None),
            P("fsdp"),
            P("fsdp", "tp"),
            P("fsdp", "tp"),
            P("fsdp", "tp"),
            P("fsdp"),
            P("fsdp"),
            P("tp", "fsdp"),
            P("fsdp"),
            P("fsdp", "tp"),
            P("fsdp", "tp"),
            P("tp", "fsdp"),
        ),
        check_vma=False,
    )
```

```python
import functools
import math

import jax
import jax.numpy as jnp
from jax import lax
from jax.experimental import pallas as pl
from jax.experimental.pallas import tpu as pltpu
from jax.sharding import PartitionSpec as P

EPS = 1e-05
THETA = 1000000.0
NEGATIVE = -1e30


def rms_scale(field_in, gain_vec):
    return (
        field_in * lax.rsqrt(jnp.mean(field_in * field_in, axis=-1, keepdims=True) + EPS) * gain_vec
    )


def rotate(field_in, positions):
    half_dim = field_in.shape[-1] // 2
    frequency = THETA ** (-(2.0 * jnp.arange(half_dim, dtype=jnp.float32)) / field_in.shape[-1])
    angles = positions[:, None] * frequency[None, :]
    cos_part = jnp.cos(angles)[:, None, :]
    sin_part = jnp.sin(angles)[:, None, :]
    lower_half = field_in[..., :half_dim]
    upper_half = field_in[..., half_dim:]
    return jnp.concatenate(
        [
            lower_half * cos_part - upper_half * sin_part,
            upper_half * cos_part + lower_half * sin_part,
        ],
        axis=-1,
    )


def linear(left_mat, right_mat):
    return jnp.dot(left_mat, right_mat, preferred_element_type=jnp.float32)


def linear_left(left_mat, right_mat):
    return lax.dot_general(
        left_mat, right_mat, (((0,), (0,)), ((), ())), preferred_element_type=jnp.float32
    )


def linear_right(left_mat, right_mat):
    return lax.dot_general(
        left_mat, right_mat, (((1,), (1,)), ((), ())), preferred_element_type=jnp.float32
    )


def swiglu(gate_act, up_act):
    return jax.nn.silu(gate_act) * up_act


def per_device_any(
    tokens,
    teacher,
    lengths,
    attn_gain,
    q_weight,
    k_weight,
    v_weight,
    q_gain,
    k_gain,
    o_weight,
    ffn_gain,
    gate_weight,
    up_weight,
    down_weight,
):
    (
        gain_one,
        w_query,
        w_key,
        w_value,
        gain_query,
        gain_key,
        w_output,
        gain_two,
        w_gate,
        w_upper,
        w_down,
    ) = (
        lax.all_gather(attn_gain, "fsdp", axis=0, tiled=True),
        lax.all_gather(q_weight, "fsdp", axis=0, tiled=True),
        lax.all_gather(k_weight, "fsdp", axis=0, tiled=True),
        lax.all_gather(v_weight, "fsdp", axis=0, tiled=True),
        lax.all_gather(q_gain, "fsdp", axis=0, tiled=True),
        lax.all_gather(k_gain, "fsdp", axis=0, tiled=True),
        lax.all_gather(o_weight, "fsdp", axis=1, tiled=True),
        lax.all_gather(ffn_gain, "fsdp", axis=0, tiled=True),
        lax.all_gather(gate_weight, "fsdp", axis=0, tiled=True),
        lax.all_gather(up_weight, "fsdp", axis=0, tiled=True),
        lax.all_gather(down_weight, "fsdp", axis=1, tiled=True),
    )
    rows_dev, block_len, model_width = tokens.shape
    count_tok = rows_dev * block_len
    head_dim = gain_query.shape[0]
    q_heads = w_query.shape[1] // head_dim
    kv_heads = w_key.shape[1] // head_dim
    group_size = q_heads // kv_heads
    score_scale = head_dim ** (-0.5)
    row_len = block_len * lax.axis_size("ctx")
    key_block = math.gcd(row_len, 512)
    block_start = lax.axis_index("ctx") * block_len
    tiles_used = (block_start + block_len + key_block - 1) // key_block
    slot_pos = block_start + jnp.arange(block_len, dtype=jnp.int32)
    positions = slot_pos.astype(jnp.float32)
    valid = (slot_pos[None, :] < lengths[:, None]).astype(jnp.float32)
    slots = count_tok * lax.axis_size("fsdp") * lax.axis_size("ctx")
    gain_two_f = gain_two.astype(jnp.float32)
    gain_one_f = gain_one.astype(jnp.float32)
    inputs = tokens.astype(jnp.float32)
    normed_one, back_one = jax.vjp(rms_scale, inputs, gain_one_f)
    normed_low = normed_one.astype(jnp.bfloat16).reshape(count_tok, model_width)
    query_raw = linear(normed_low, w_query)
    key_raw = linear(normed_low, w_key)
    value_raw = linear(normed_low, w_value)

    def heads_post(raw_heads, gain_vec):
        shaped = raw_heads.reshape(rows_dev, block_len, -1, head_dim)
        return rotate(rms_scale(shaped, gain_vec), positions)

    query_rot, query_back = jax.vjp(heads_post, query_raw, gain_query.astype(jnp.float32))
    key_rot, key_back = jax.vjp(heads_post, key_raw, gain_key.astype(jnp.float32))
    queries = query_rot.astype(jnp.bfloat16).reshape(
        rows_dev, block_len, kv_heads, group_size, head_dim
    )
    key_rows = key_rot.astype(jnp.bfloat16).reshape(rows_dev, block_len, kv_heads * head_dim)
    values = value_raw.astype(jnp.bfloat16).reshape(rows_dev, block_len, kv_heads * head_dim)
    keys_all, values_all = (
        lax.all_gather(key_rows, "ctx", axis=1, tiled=True),
        lax.all_gather(values, "ctx", axis=1, tiled=True),
    )

    def key_tile(tile_index):
        tile_start = tile_index * key_block
        key_pos = tile_start + jnp.arange(key_block, dtype=jnp.int32)
        key_part = lax.dynamic_slice_in_dim(keys_all, tile_start, key_block, 1).reshape(
            rows_dev, key_block, kv_heads, head_dim
        )
        value_part = lax.dynamic_slice_in_dim(values_all, tile_start, key_block, 1).reshape(
            rows_dev, key_block, kv_heads, head_dim
        )
        scores = (
            jnp.einsum("rqhgd,rkhd->rhgqk", queries, key_part, preferred_element_type=jnp.float32)
            * score_scale
        )
        allowed = (key_pos[None, None, :] <= slot_pos[None, :, None]) & (
            key_pos[None, None, :] < lengths[:, None, None]
        )
        return (tile_start, scores, allowed[:, None, None], key_part, value_part)

    stat_shape = (rows_dev, kv_heads, group_size, block_len)

    def stats_step(tile_index, carried):
        running_max, running_sum = carried
        tile_start, scores, allowed, key_part, value_part = key_tile(tile_index)
        masked = jnp.where(allowed, scores, NEGATIVE)
        new_max = jnp.maximum(running_max, jnp.max(masked, axis=-1))
        terms = jnp.where(allowed, jnp.exp(masked - new_max[..., None]), 0.0)
        return (new_max, running_sum * jnp.exp(running_max - new_max) + jnp.sum(terms, axis=-1))

    running_max, running_sum = lax.fori_loop(
        0,
        tiles_used,
        stats_step,
        (jnp.full(stat_shape, NEGATIVE, jnp.float32), jnp.zeros(stat_shape, jnp.float32)),
    )
    log_total = running_max + jnp.log(running_sum)
    out_shape = (rows_dev, block_len, kv_heads, group_size, head_dim)

    def value_step(tile_index, carried):
        rounded_out, exact_out = carried
        tile_start, scores, allowed, key_part, value_part = key_tile(tile_index)
        tile_probs = jnp.where(allowed, jnp.exp(scores - log_total[..., None]), 0.0)
        rounded_out = rounded_out + jnp.einsum(
            "rhgqk,rkhd->rqhgd",
            tile_probs.astype(jnp.bfloat16),
            value_part,
            preferred_element_type=jnp.float32,
        )
        exact_out = exact_out + jnp.einsum(
            "rhgqk,rkhd->rqhgd", tile_probs, value_part.astype(jnp.float32)
        )
        return (rounded_out, exact_out)

    rounded_out, exact_out = lax.fori_loop(
        0,
        tiles_used,
        value_step,
        (jnp.zeros(out_shape, jnp.float32), jnp.zeros(out_shape, jnp.float32)),
    )
    attended = rounded_out.astype(jnp.bfloat16).reshape(count_tok, q_heads * head_dim)
    attn_total = lax.psum(linear(attended, w_output), "tp")
    resid = inputs + attn_total.reshape(rows_dev, block_len, model_width)
    normed_two, back_two = jax.vjp(rms_scale, resid, gain_two_f)
    normed_second = normed_two.astype(jnp.bfloat16).reshape(count_tok, model_width)
    gate_act = linear(normed_second, w_gate)
    up_act = linear(normed_second, w_upper)
    hidden_full, back_glu = jax.vjp(swiglu, gate_act, up_act)
    hidden = hidden_full.astype(jnp.bfloat16)
    ffn_total = lax.psum(linear(hidden, w_down), "tp")
    result = resid + ffn_total.reshape(rows_dev, block_len, model_width)
    error_value = result - teacher.astype(jnp.float32)
    valid_col = valid[..., None]
    total_square, total_count = lax.psum(
        (jnp.sum(valid_col * error_value * error_value), jnp.sum(valid)), ("fsdp", "ctx")
    )
    teacher_loss = total_square / (total_count * model_width)
    grad_result = valid_col * error_value * (slots / total_count)
    grad_low = grad_result.astype(jnp.bfloat16).reshape(count_tok, model_width)
    grad_down = linear_left(hidden, grad_low)
    grad_hidden = linear_right(grad_low, w_down)
    grad_gate_full, grad_up_full = back_glu(grad_hidden)
    grad_gate = grad_gate_full.astype(jnp.bfloat16)
    grad_up = grad_up_full.astype(jnp.bfloat16)
    grad_wgate = linear_left(normed_second, grad_gate)
    grad_wup = linear_left(normed_second, grad_up)
    normed_two_part = linear_right(grad_gate, w_gate) + linear_right(grad_up, w_upper)
    grad_normed_two = lax.psum(normed_two_part, "tp")
    grad_resid_norm, grad_gain_two = back_two(
        grad_normed_two.reshape(rows_dev, block_len, model_width)
    )
    grad_resid = grad_result + grad_resid_norm
    grad_attn_low = grad_resid.astype(jnp.bfloat16).reshape(count_tok, model_width)
    grad_woutput = linear_left(attended, grad_attn_low)
    grad_attended = linear_right(grad_attn_low, w_output).astype(jnp.bfloat16).reshape(out_shape)
    delta = jnp.einsum("rqhgd,rqhgd->rhgq", grad_attended.astype(jnp.float32), exact_out)
    full_shape = (rows_dev, row_len, kv_heads * head_dim)

    def grad_step(tile_index, carried):
        grad_queries, grad_keys, grad_values = carried
        tile_start, scores, allowed, key_part, value_part = key_tile(tile_index)
        tile_probs = jnp.where(allowed, jnp.exp(scores - log_total[..., None]), 0.0)
        grad_probs = jnp.einsum(
            "rqhgd,rkhd->rhgqk", grad_attended, value_part, preferred_element_type=jnp.float32
        )
        grad_scores = (tile_probs * (grad_probs - delta[..., None])).astype(jnp.bfloat16)
        grad_queries = (
            grad_queries
            + jnp.einsum(
                "rhgqk,rkhd->rqhgd", grad_scores, key_part, preferred_element_type=jnp.float32
            )
            * score_scale
        )
        key_term = (
            jnp.einsum(
                "rhgqk,rqhgd->rkhd", grad_scores, queries, preferred_element_type=jnp.float32
            )
            * score_scale
        )
        value_term = jnp.einsum(
            "rhgqk,rqhgd->rkhd",
            tile_probs.astype(jnp.bfloat16),
            grad_attended,
            preferred_element_type=jnp.float32,
        )
        grad_keys = lax.dynamic_update_slice_in_dim(
            grad_keys, key_term.reshape(rows_dev, key_block, kv_heads * head_dim), tile_start, 1
        )
        grad_values = lax.dynamic_update_slice_in_dim(
            grad_values, value_term.reshape(rows_dev, key_block, kv_heads * head_dim), tile_start, 1
        )
        return (grad_queries, grad_keys, grad_values)

    grad_queries, grad_keys, grad_values = lax.fori_loop(
        0,
        tiles_used,
        grad_step,
        (
            jnp.zeros(out_shape, jnp.float32),
            jnp.zeros(full_shape, jnp.float32),
            jnp.zeros(full_shape, jnp.float32),
        ),
    )
    key_grad, value_grad = (
        lax.psum_scatter(grad_keys, "ctx", scatter_dimension=1, tiled=True),
        lax.psum_scatter(grad_values, "ctx", scatter_dimension=1, tiled=True),
    )
    grad_query_raw, grad_gain_query = query_back(
        grad_queries.reshape(rows_dev, block_len, q_heads, head_dim)
    )
    grad_key_raw, grad_gain_key = key_back(
        key_grad.reshape(rows_dev, block_len, kv_heads, head_dim)
    )
    query_low = grad_query_raw.astype(jnp.bfloat16)
    key_low = grad_key_raw.astype(jnp.bfloat16)
    value_low = value_grad.reshape(count_tok, kv_heads * head_dim).astype(jnp.bfloat16)
    grad_wquery = linear_left(normed_low, query_low)
    grad_wkey = linear_left(normed_low, key_low)
    grad_wvalue = linear_left(normed_low, value_low)
    normed_part = (
        linear_right(query_low, w_query)
        + linear_right(key_low, w_key)
        + linear_right(value_low, w_value)
    )
    grad_normed_one, grad_gain_query, grad_gain_key = lax.psum(
        (normed_part, grad_gain_query, grad_gain_key), "tp"
    )
    grad_input_norm, grad_gain_one = back_one(
        grad_normed_one.reshape(rows_dev, block_len, model_width)
    )
    tokens_grad = grad_resid + grad_input_norm
    partials = (
        grad_gain_one,
        grad_wquery,
        grad_wkey,
        grad_wvalue,
        grad_gain_query,
        grad_gain_key,
        grad_woutput,
        grad_gain_two,
        grad_wgate,
        grad_wup,
        grad_down,
    )
    pieces = (
        lax.psum_scatter(partials[0], ("fsdp", "ctx"), scatter_dimension=0, tiled=True),
        lax.psum_scatter(partials[1], ("fsdp", "ctx"), scatter_dimension=0, tiled=True),
        lax.psum_scatter(partials[2], ("fsdp", "ctx"), scatter_dimension=0, tiled=True),
        lax.psum_scatter(partials[3], ("fsdp", "ctx"), scatter_dimension=0, tiled=True),
        lax.psum_scatter(partials[4], ("fsdp", "ctx"), scatter_dimension=0, tiled=True),
        lax.psum_scatter(partials[5], ("fsdp", "ctx"), scatter_dimension=0, tiled=True),
        lax.psum_scatter(partials[6], ("fsdp", "ctx"), scatter_dimension=1, tiled=True),
        lax.psum_scatter(partials[7], ("fsdp", "ctx"), scatter_dimension=0, tiled=True),
        lax.psum_scatter(partials[8], ("fsdp", "ctx"), scatter_dimension=0, tiled=True),
        lax.psum_scatter(partials[9], ("fsdp", "ctx"), scatter_dimension=0, tiled=True),
        lax.psum_scatter(partials[10], ("fsdp", "ctx"), scatter_dimension=1, tiled=True),
    )
    summed = (
        lax.all_gather(pieces[0], "ctx", axis=0, tiled=True),
        lax.all_gather(pieces[1], "ctx", axis=0, tiled=True),
        lax.all_gather(pieces[2], "ctx", axis=0, tiled=True),
        lax.all_gather(pieces[3], "ctx", axis=0, tiled=True),
        lax.all_gather(pieces[4], "ctx", axis=0, tiled=True),
        lax.all_gather(pieces[5], "ctx", axis=0, tiled=True),
        lax.all_gather(pieces[6], "ctx", axis=1, tiled=True),
        lax.all_gather(pieces[7], "ctx", axis=0, tiled=True),
        lax.all_gather(pieces[8], "ctx", axis=0, tiled=True),
        lax.all_gather(pieces[9], "ctx", axis=0, tiled=True),
        lax.all_gather(pieces[10], "ctx", axis=1, tiled=True),
    )
    return (
        result.astype(jnp.bfloat16),
        teacher_loss,
        tokens_grad,
        summed[0],
        summed[1],
        summed[2],
        summed[3],
        summed[4],
        summed[5],
        summed[6],
        summed[7],
        summed[8],
        summed[9],
        summed[10],
    )


BF16 = jnp.bfloat16
F32 = jnp.float32
LOG2E = math.log2(math.e)
X_SWAP = [(0, 2), (2, 0), (1, 3), (3, 1)]
CORE_SWAP = [(0, 1), (1, 0), (2, 3), (3, 2)]
Y_SWAP = [(0, 1), (1, 0)]
Z_UP = [(0, 1), (1, 2), (2, 3), (3, 0)]
Z_DOWN = [(0, 3), (1, 0), (2, 1), (3, 2)]
Z_NEAR = [(0, 1), (1, 0), (2, 3), (3, 2)]
Z_FAR = [(0, 2), (2, 0), (1, 3), (3, 1)]
MASKS = (0, 2, 1, 3)
ANY = pl.BlockSpec(memory_space=pl.ANY)
SMEM = pl.BlockSpec(memory_space=pltpu.SMEM)


def fits(mesh):
    return dict(mesh.shape) == {"fsdp": 4, "ctx": 2, "tp": 4}


def dot(left, right, left_dim, right_dim):
    return lax.dot_general(
        left, right, (((left_dim,), (right_dim,)), ((), ())), preferred_element_type=F32
    )


def sigmoid(v):
    return 0.5 * jnp.tanh(0.5 * v) + 0.5


def whole(shape):
    zeros = (0,) * len(shape)
    return pl.BlockSpec(shape, lambda *_: zeros, pipeline_mode=pl.Buffered(1))


def settings(dims, mib):
    return pltpu.CompilerParams(
        dimension_semantics=("arbitrary",) * dims, vmem_limit_bytes=mib << 20
    )


def shape_of(shape, dtype):
    return jax.ShapeDtypeStruct(shape, dtype)


def cost(large, microseconds=None):
    size = 1 << 42 if large else 1 << 10
    if microseconds is not None:
        size = int(microseconds * 1.15e9)
    return pl.CostEstimate(flops=size, bytes_accessed=size >> 12, transcendentals=0)


def pack_kernel(info, o_in, g_in, u_in, d_in, *refs):
    out_ref, ffn_ref, *chunk_refs, others_ref, o_ref, g_ref, u_ref, d_ref, sems = refs
    ctx = info[2]
    pairs = ((o_in, o_ref), (g_in, g_ref), (u_in, u_ref), (d_in, d_ref))
    copies = [pltpu.make_async_copy(a, b, sems.at[i]) for i, (a, b) in enumerate(pairs)]
    for copy in copies:
        copy.start()
    for copy in copies:
        copy.wait()
    out_ref[...] = o_ref[...].astype(F32).T.astype(BF16)
    third = g_ref.shape[1] // 3
    for j in range(3):
        at = pl.multiple_of(jnp.where(ctx == 0, j, 2 - j) * third, third)
        parts = [
            g_ref[:, pl.ds(at, third)],
            u_ref[:, pl.ds(at, third)],
            d_ref[pl.ds(at, third), :].astype(F32).T.astype(BF16),
        ]
        for i, part in enumerate(parts):
            chunk_refs[j][:, i * third : (i + 1) * third] = part
            if j:
                others_ref[:, (3 * j - 3 + i) * third : (3 * j - 2 + i) * third] = part
            ffn_ref[:, (3 * j + i) * third : (3 * j + i + 1) * third] = part


def pack(info, o, g, u, d):
    rows, units = g.shape
    feats = o.shape[0]
    widths = (feats, 3 * units, units, units, units, 2 * units)
    return pl.pallas_call(
        pack_kernel,
        in_specs=[SMEM] + [ANY] * 4,
        out_specs=[pl.BlockSpec(memory_space=pltpu.VMEM)] * 6,
        out_shape=[shape_of((rows, n), BF16) for n in widths],
        scratch_shapes=[pltpu.VMEM(a.shape, BF16) for a in (o, g, u, d)]
        + [pltpu.SemaphoreType.DMA((4,))],
        compiler_params=pltpu.CompilerParams(vmem_limit_bytes=24 << 20),
        cost_estimate=cost(False),
        name="pack",
    )(info, o, g, u, d)


def join_kernel(q_ref, k_ref, v_ref, out_ref):
    at = 0
    for ref in (q_ref, k_ref, v_ref):
        out_ref[:, at : at + ref.shape[1]] = ref[...]
        at += ref.shape[1]


def join(q, k, v):
    return pl.pallas_call(
        join_kernel,
        out_shape=shape_of((q.shape[0], q.shape[1] + k.shape[1] + v.shape[1]), BF16),
        compiler_params=pltpu.CompilerParams(vmem_limit_bytes=8 << 20),
        cost_estimate=cost(False),
        name="join",
    )(q, k, v)


def norm_one_kernel(info, tok_ref, gain_ref, x_ref, nt_ref, x32):
    quarter = x_ref.shape[1] // 4
    for p, mask in enumerate(MASKS):
        at = pl.multiple_of(jnp.bitwise_xor(info[1], mask) * quarter, quarter)
        part = tok_ref[0, :, pl.ds(at, quarter)]
        x_ref[:, p * quarter : (p + 1) * quarter] = part
        x32[:, p * quarter : (p + 1) * quarter] = part.astype(F32)
    x = x32[...]
    rho = lax.rsqrt(jnp.mean(x * x, axis=-1, keepdims=True) + EPS)
    nt_ref[...] = (x * rho * gain_ref[...]).T.astype(BF16)


def norm_one(info, tokens, gain, tile):
    _, tok, width = tokens.shape
    return pl.pallas_call(
        norm_one_kernel,
        grid_spec=pltpu.PrefetchScalarGridSpec(
            num_scalar_prefetch=1,
            grid=(tok // tile,),
            in_specs=[
                pl.BlockSpec((1, tile, width), lambda i, info: (info[0], i, 0)),
                pl.BlockSpec((1, width), lambda i, info: (0, 0)),
            ],
            out_specs=[
                pl.BlockSpec((tile, width), lambda i, info: (i, 0)),
                pl.BlockSpec((width, tile), lambda i, info: (0, i)),
            ],
            scratch_shapes=[pltpu.VMEM((tile, width), F32)],
        ),
        out_shape=[shape_of((tok, width), BF16), shape_of((width, tok), BF16)],
        compiler_params=settings(1, 24),
        cost_estimate=cost(False),
        name="norm_one",
    )(info, tokens, gain)


def proj_kernel(heads, block, plan, count, info, *refs):
    nt_ref, cos_ref, sin_ref, qg_ref, kg_ref, rot_ref, raw_ref, w_ref, sem = refs[count:]
    rows = w_ref.shape[0] // 4

    @pl.when(pl.program_id(0) == 0)
    def _():
        for k in range(4):

            @pl.when(block(info) == k)
            def _():
                for p, (piece, row) in enumerate(plan[k]):
                    src = refs[piece].at[pl.ds(row, rows)]
                    pltpu.make_async_copy(src, w_ref.at[pl.ds(p * rows, rows)], sem).start()

        pltpu.make_async_copy(w_ref, w_ref, sem).wait()

    hd = qg_ref.shape[0]
    half = hd // 2
    raw = dot(w_ref[...], nt_ref[...], 0, 0)
    cos_part, sin_part = cos_ref[...], sin_ref[...]
    heads_q, heads_k = heads
    raw_ref[...] = raw.astype(BF16)
    for h in range(heads_q + heads_k):
        v = raw[h * hd : (h + 1) * hd]
        rho = lax.rsqrt(jnp.mean(v * v, axis=0, keepdims=True) + EPS)
        v = v * rho * (qg_ref[...] if h < heads_q else kg_ref[...])
        a, b = v[:half], v[half:]
        rot_ref[h * hd : h * hd + half, :] = (a * cos_part - b * sin_part).astype(BF16)
        rot_ref[h * hd + half : (h + 1) * hd, :] = (b * cos_part + a * sin_part).astype(BF16)
    at = (heads_q + heads_k) * hd
    rot_ref[at:, :] = raw[at:].astype(BF16)


def project(info, weights, normed_t, cos_part, sin_part, gain_q, gain_k, heads, block):
    plan, pieces = weights
    width, tok = normed_t.shape
    cols = pieces[0].shape[1]
    tile = min(512, tok)
    const = lambda a: pl.BlockSpec(a.shape, lambda i, info: (0, 0))
    tab = lambda a: pl.BlockSpec((a.shape[0], tile), lambda i, info: (0, i))
    return pl.pallas_call(
        functools.partial(proj_kernel, heads, block, plan, len(pieces)),
        grid_spec=pltpu.PrefetchScalarGridSpec(
            num_scalar_prefetch=1,
            grid=(tok // tile,),
            in_specs=[ANY] * len(pieces)
            + [tab(normed_t), tab(cos_part), tab(sin_part), const(gain_q), const(gain_k)],
            out_specs=[pl.BlockSpec((cols, tile), lambda i, info: (0, i))] * 2,
            scratch_shapes=[pltpu.VMEM((width, cols), BF16), pltpu.SemaphoreType.DMA],
        ),
        out_shape=[shape_of((cols, tok), BF16), shape_of((cols, tok), BF16)],
        compiler_params=settings(1, 24),
        cost_estimate=cost(False),
        name="project",
    )(info, *pieces, normed_t, cos_part, sin_part, gain_q, gain_k)


def head_back_kernel(
    heads, info, dm_ref, dt_ref, rm_ref, rt_ref, cos_ref, sin_ref, qg_ref, kg_ref, out_ref, gg_ref
):
    step, part = pl.program_id(0), pl.program_id(1)
    hd = qg_ref.shape[0]
    half = hd // 2
    heads_q, heads_k = heads
    cos_part, sin_part = cos_ref[...], sin_ref[...]
    tile = cos_part.shape[1]

    @pl.when((step == 0) & (part == 0))
    def _():
        gg_ref[...] = jnp.zeros_like(gg_ref)

    def work(d_ref, r_ref):
        gain_q = jnp.zeros((hd, 1), F32)
        gain_k = jnp.zeros((hd, 1), F32)
        done = []
        for h in range(heads_q + heads_k):
            is_q = h < heads_q
            g = d_ref[h * hd : (h + 1) * hd, :].astype(F32)
            raw = r_ref[h * hd : (h + 1) * hd, :].astype(F32)
            a, b = g[:half], g[half:]
            turned = jnp.concatenate(
                [a * cos_part + b * sin_part, b * cos_part - a * sin_part], axis=0
            )
            rho = lax.rsqrt(jnp.mean(raw * raw, axis=0, keepdims=True) + EPS)
            unit = raw * rho
            prod = turned * unit
            scaled = turned * (qg_ref[...] if is_q else kg_ref[...])
            mean = jnp.mean(scaled * unit, axis=0, keepdims=True)
            done.append(rho * (scaled - unit * mean))
            total = jnp.sum(prod, axis=1, keepdims=True)
            if is_q:
                gain_q = gain_q + total
            else:
                gain_k = gain_k + total
        done.append(d_ref[(heads_q + heads_k) * hd :, :].astype(F32))
        out_ref[0] = jnp.concatenate(done, axis=0).T.astype(BF16)
        lane = lax.broadcasted_iota(jnp.int32, gg_ref.shape, 1)
        gg_ref[...] += jnp.where(lane == 0, gain_q, jnp.where(lane == 1, gain_k, 0.0))

    @pl.when(step == 0)
    def _():
        work(dm_ref, rm_ref)

    @pl.when(step == 1)
    def _():
        work(dt_ref, rt_ref)


def head_back(info, grad_mine, grad_theirs, raw_mine, raw_theirs, cos_part, sin_part, gq, gk, heads):
    cols, tok = grad_mine.shape
    tile = min(512, tok)
    mine = pl.BlockSpec((cols, tile), lambda s, i, info: (0, jnp.where(s == 0, i, tok // tile - 1)))
    theirs = pl.BlockSpec((cols, tile), lambda s, i, info: (0, jnp.where(s == 0, 0, i)))
    tab = lambda a: pl.BlockSpec((a.shape[0], tile), lambda s, i, info: (0, i))
    const = lambda a: pl.BlockSpec(a.shape, lambda s, i, info: (0, 0))
    return pl.pallas_call(
        functools.partial(head_back_kernel, heads),
        grid_spec=pltpu.PrefetchScalarGridSpec(
            num_scalar_prefetch=1,
            grid=(2, tok // tile),
            in_specs=[
                mine,
                theirs,
                mine,
                theirs,
                tab(cos_part),
                tab(sin_part),
                const(gq),
                const(gk),
            ],
            out_specs=[
                pl.BlockSpec(
                    (1, tile, cols), lambda s, i, info: (jnp.bitwise_xor(info[2], s), i, 0)
                ),
                pl.BlockSpec((gq.shape[0], 128), lambda s, i, info: (0, 0)),
            ],
        ),
        out_shape=[shape_of((2, tok, cols), BF16), shape_of((gq.shape[0], 128), F32)],
        compiler_params=settings(2, 60),
        cost_estimate=cost(False),
        name="head_back",
    )(info, grad_mine, grad_theirs, raw_mine, raw_theirs, cos_part, sin_part, gq, gk)


def load_rows(info, mine_ref, got_ref, rows, sems):
    tok = mine_ref.shape[1]
    ctx = info[2]
    here = pl.multiple_of(ctx * tok, tok)
    there = pl.multiple_of((1 - ctx) * tok, tok)
    one = pltpu.make_async_copy(mine_ref, rows.at[:, pl.ds(here, tok)], sems.at[0])
    two = pltpu.make_async_copy(got_ref, rows.at[:, pl.ds(there, tok)], sems.at[1])
    one.start()
    two.start()
    one.wait()
    two.wait()


def keys_with_bias(keys, length):
    hd, slots = keys.shape
    pos = lax.broadcasted_iota(jnp.int32, (hd, slots), 1)
    row = lax.broadcasted_iota(jnp.int32, (hd, slots), 0)
    bias = jnp.where((row == 0) & (pos >= length), NEGATIVE, 0.0)
    return jnp.concatenate([keys.astype(F32), bias], axis=0).T.astype(BF16)


def query_with_one(pair):
    one_row = jnp.where(lax.broadcasted_iota(jnp.int32, pair.shape, 0) == 0, 1.0, 0.0)
    return jnp.concatenate([pair, one_row.astype(BF16)], axis=0)


def by_halves(left, right):
    half = left.shape[1] // 2
    return jnp.concatenate(
        [left[:, :half], right[:, :half], left[:, half:], right[:, half:]], axis=1
    )


def by_heads(both):
    quarter = both.shape[1] // 4
    part = lambda i: both[:, i * quarter : (i + 1) * quarter]
    return (
        jnp.concatenate([part(0), part(2)], axis=1),
        jnp.concatenate([part(1), part(3)], axis=1),
    )


def causal(scores):
    half = scores.shape[0]
    key_pos = lax.broadcasted_iota(jnp.int32, (half, half), 0)
    query_pos = lax.broadcasted_iota(jnp.int32, (half, half), 1)
    allowed = key_pos <= query_pos
    return jnp.where(jnp.concatenate([allowed, allowed], axis=1), scores, NEGATIVE)


def attn_fwd_kernel(
    width, hd, info, mine_ref, got_ref, keep_ref, send_ref, lse_ref, rows, key_rows, sems
):
    head, block = pl.program_id(0), pl.program_id(1)
    heads_k = pl.num_programs(0)
    scale = hd**-0.5 * LOG2E
    length = info[3]
    key_at = pl.multiple_of(heads_k * 2 * hd + head * hd, hd)
    value_at = pl.multiple_of(heads_k * 3 * hd + head * hd, hd)
    query_at = pl.multiple_of(head * 2 * hd, 2 * hd)

    @pl.when((head == 0) & (block == 0))
    def _():
        load_rows(info, mine_ref, got_ref, rows, sems)

    @pl.when(block == 0)
    def _():
        key_rows[...] = keys_with_bias(rows[pl.ds(key_at, hd), :], length)

    start = pl.multiple_of(block * width, width)
    both = rows[pl.ds(query_at, 2 * hd), pl.ds(start, width)]
    query = query_with_one(by_halves(both[:hd], both[hd:]))

    def tile(at, carried, diagonal):
        out, total = carried
        scores = dot(key_rows[pl.ds(at, width), :], query, 1, 0)
        if diagonal:
            key_pos = lax.broadcasted_iota(jnp.int32, (width, width), 0)
            query_pos = lax.broadcasted_iota(jnp.int32, (width, width), 1)
            allowed = key_pos <= query_pos
            allowed = by_halves(allowed, allowed)
            scores = jnp.where(allowed, scores, NEGATIVE)
        probs = jnp.exp2(scores * scale)
        total = total + jnp.sum(probs, axis=0, keepdims=True)
        out = out + dot(rows[pl.ds(value_at, hd), pl.ds(at, width)], probs.astype(BF16), 1, 0)
        return out, total

    carried = (jnp.zeros((hd, 2 * width), F32), jnp.zeros((1, 2 * width), F32))
    full = jnp.minimum(block, lax.div(length + width - 1, width))
    carried = lax.fori_loop(
        0, full, lambda j, c: tile(pl.multiple_of(j * width, width), c, False), carried
    )
    out, total = tile(start, carried, True)
    out = out * (1.0 / total)
    out = jnp.concatenate(by_heads(out), axis=0).T.astype(BF16)
    here = block // 2 == info[2]

    @pl.when(here)
    def _():
        keep_ref[...] = out

    @pl.when(jnp.logical_not(here))
    def _():
        send_ref[...] = out

    log_first, log_second = by_heads(jnp.log2(total))
    lse_ref[0, 0:1, :] = log_first
    lse_ref[0, 1:2, :] = log_second


def keep_block(i, info):
    return jnp.clip(i - 2 * info[2], 0, 1)


def send_block(i, info):
    return jnp.clip(i - 2 * (1 - info[2]), 0, 1)


def attn_fwd(info, mine, got, hd):
    cols, tok = mine.shape
    heads_k = cols // (4 * hd)
    width = tok // 2
    return pl.pallas_call(
        functools.partial(attn_fwd_kernel, width, hd),
        grid_spec=pltpu.PrefetchScalarGridSpec(
            num_scalar_prefetch=1,
            grid=(heads_k, 4),
            in_specs=[ANY, ANY],
            out_specs=[
                pl.BlockSpec((width, 2 * hd), lambda h, i, info: (keep_block(i, info), h)),
                pl.BlockSpec((width, 2 * hd), lambda h, i, info: (send_block(i, info), h)),
                pl.BlockSpec((1, 2, width), lambda h, i, info: (h, 0, i)),
            ],
            scratch_shapes=[
                pltpu.VMEM((cols, 2 * tok), BF16),
                pltpu.VMEM((2 * tok, 2 * hd), BF16),
                pltpu.SemaphoreType.DMA((2,)),
            ],
        ),
        out_shape=[
            shape_of((tok, heads_k * 2 * hd), BF16),
            shape_of((tok, heads_k * 2 * hd), BF16),
            shape_of((heads_k, 2, 2 * tok), F32),
        ],
        compiler_params=settings(2, 60),
        cost_estimate=cost(True),
        name="attn_fwd",
    )(info, mine, got)


def attn_bwd_kernel(
    width,
    hd,
    info,
    mine_ref,
    got_ref,
    ok_ref,
    os_ref,
    gk_ref,
    gs_ref,
    lse_ref,
    keep_ref,
    send_ref,
    rows,
    key_rows,
    value_rows,
    key_sum,
    value_sum,
    sems,
):
    head, block = pl.program_id(0), pl.program_id(1)
    heads_k = pl.num_programs(0)
    scale = hd**-0.5
    length = info[3]
    ctx = info[2]
    tok = keep_ref.shape[1]
    key_at = pl.multiple_of(heads_k * 2 * hd + head * hd, hd)
    value_at = pl.multiple_of(heads_k * 3 * hd + head * hd, hd)
    query_at = pl.multiple_of(head * 2 * hd, 2 * hd)

    @pl.when((head == 0) & (block == 0))
    def _():
        load_rows(info, mine_ref, got_ref, rows, sems)

    @pl.when(block == 0)
    def _():
        key_rows[...] = keys_with_bias(rows[pl.ds(key_at, hd), :], length)
        value_rows[...] = rows[pl.ds(value_at, hd), :].astype(F32).T.astype(BF16)
        key_sum[...] = jnp.zeros_like(key_sum)
        value_sum[...] = jnp.zeros_like(value_sum)

    start = pl.multiple_of(block * width, width)
    here = block // 2 == ctx

    def store_query(value):
        at = pl.ds(pl.multiple_of((block % 2) * width, width), width)

        @pl.when(here)
        def _():
            keep_ref[pl.ds(query_at, 2 * hd), at] = value

        @pl.when(jnp.logical_not(here))
        def _():
            send_ref[pl.ds(query_at, 2 * hd), at] = value

    @pl.when(block * width < length)
    def _():
        both = rows[pl.ds(query_at, 2 * hd), pl.ds(start, width)]
        pair = by_halves(both[:hd], both[hd:])
        query = query_with_one(pair)
        query_rows = pair.astype(F32).T.astype(BF16)
        grad_wide = jnp.where(here, gk_ref[...].astype(F32), gs_ref[...].astype(F32))
        out_wide = jnp.where(here, ok_ref[...].astype(F32), os_ref[...].astype(F32))
        grad_t = grad_wide.T
        prod = (grad_wide * out_wide).T
        grad = by_halves(grad_t[:hd], grad_t[hd:]).astype(BF16)
        half = width // 2
        grad_rows = jnp.concatenate(
            [
                grad_wide[:half, :hd],
                grad_wide[:half, hd:],
                grad_wide[half:, :hd],
                grad_wide[half:, hd:],
            ],
            axis=0,
        ).astype(BF16)
        delta = by_halves(
            jnp.sum(prod[:hd], axis=0, keepdims=True), jnp.sum(prod[hd:], axis=0, keepdims=True)
        )
        lse = by_halves(lse_ref[0, 0:1, :], lse_ref[0, 1:2, :])

        def terms(at, keys, first, mask):
            scores = dot(key_rows[pl.ds(at, keys), :], query[:, first:], 1, 0)
            if mask:
                part = causal(scores[:, :width])
                wide = scores.shape[1] > width
                scores = jnp.concatenate([part, scores[:, width:]], axis=1) if wide else part
            probs = jnp.exp2(scores * (scale * LOG2E) - lse[:, first:])
            grad_probs = dot(value_rows[pl.ds(at, keys), :], grad[:, first:], 1, 0)
            grad_scores = (probs * (grad_probs - delta[:, first:])).astype(BF16)
            value_sum[pl.ds(at, keys), :] += dot(probs.astype(BF16), grad_rows[first:], 1, 0)
            key_sum[pl.ds(at, keys), :] += dot(grad_scores, query_rows[first:], 1, 0)
            return dot(rows[pl.ds(key_at, hd), pl.ds(at, keys)], grad_scores, 1, 0)

        query_sum = lax.fori_loop(
            0,
            block,
            lambda j, s: s + terms(pl.multiple_of(j * width, width), width, 0, False),
            jnp.zeros((hd, 2 * width), F32),
        )
        query_sum = query_sum + terms(start, half, 0, True)
        later = terms(pl.multiple_of(start + half, half), half, width, True)
        query_sum = jnp.concatenate([query_sum[:, :width], query_sum[:, width:] + later], axis=1)
        store_query(jnp.concatenate(by_heads(query_sum * scale), axis=0).astype(BF16))

    @pl.when(block * width >= length)
    def _():
        store_query(jnp.zeros((2 * hd, width), BF16))

    @pl.when(block == 3)
    def _():
        for at, total in ((key_at, key_sum[...] * scale), (value_at, value_sum[...])):
            total = total.T.astype(BF16)
            left, right = total[:, :tok], total[:, tok:]

            @pl.when(ctx == 0)
            def _():
                keep_ref[pl.ds(at, hd), :] = left
                send_ref[pl.ds(at, hd), :] = right

            @pl.when(ctx == 1)
            def _():
                keep_ref[pl.ds(at, hd), :] = right
                send_ref[pl.ds(at, hd), :] = left


def attn_bwd(info, mine, got, out_keep, out_send, grad_keep, grad_send, lse, hd):
    cols, tok = mine.shape
    heads_k = cols // (4 * hd)
    width = tok // 2
    keep = pl.BlockSpec((width, 2 * hd), lambda h, i, info: (keep_block(i, info), h))
    send = pl.BlockSpec((width, 2 * hd), lambda h, i, info: (send_block(i, info), h))
    full = pl.BlockSpec((cols, tok), lambda h, i, info: (0, 0))
    return pl.pallas_call(
        functools.partial(attn_bwd_kernel, width, hd),
        grid_spec=pltpu.PrefetchScalarGridSpec(
            num_scalar_prefetch=1,
            grid=(heads_k, 4),
            in_specs=[
                ANY,
                ANY,
                keep,
                send,
                keep,
                send,
                pl.BlockSpec((1, 2, width), lambda h, i, info: (h, 0, i)),
            ],
            out_specs=[full, full],
            scratch_shapes=[
                pltpu.VMEM((cols, 2 * tok), BF16),
                pltpu.VMEM((2 * tok, 2 * hd), BF16),
                pltpu.VMEM((2 * tok, hd), BF16),
                pltpu.VMEM((2 * tok, hd), F32),
                pltpu.VMEM((2 * tok, hd), F32),
                pltpu.SemaphoreType.DMA((2,)),
            ],
        ),
        out_shape=[shape_of((cols, tok), BF16), shape_of((cols, tok), BF16)],
        compiler_params=settings(2, 60),
        cost_estimate=cost(True, 16.2),
        name="attn_bwd",
    )(info, mine, got, out_keep, out_send, grad_keep, grad_send, lse)


def load_blocks(plan, pieces, target, sem):
    rows = target.shape[1] // 4

    @pl.when(pl.program_id(0) == 0)
    def _():
        for k, places in enumerate(plan):
            for p, (piece, row) in enumerate(places):
                src = pieces[piece].at[pl.ds(row, rows)]
                pltpu.make_async_copy(src, target.at[k, pl.ds(p * rows, rows)], sem).start()
        pltpu.make_async_copy(target, target, sem).wait()


def out_proj_kernel(plan, count, info, *refs):
    x_ref, a0, a1, b0, b1, gain_ref, r_ref, n_ref, nt_ref, att_ref, w_ref, sem = refs[count:]
    load_blocks(plan, refs, w_ref, sem)
    ctx = info[2]
    total = x_ref[...].astype(F32)
    for j, ref, side in ((0, a0, ctx), (1, a1, ctx), (0, b0, 1 - ctx), (1, b1, 1 - ctx)):
        block = 2 * side + j
        part = ref[...]
        att_ref[block] = part
        total = total + dot(part, w_ref[block], 1, 1)
    rho = lax.rsqrt(jnp.mean(total * total, axis=-1, keepdims=True) + EPS)
    normed = total * rho * gain_ref[...]
    r_ref[...] = total
    n_ref[...] = normed.astype(BF16)
    nt_ref[...] = normed.T.astype(BF16)


def out_proj(info, x, mine, theirs, weights, gain, tile):
    plan, pieces = weights
    tok, width = x.shape
    feats = pieces[0].shape[1]
    rows_of = lambda n: pl.BlockSpec((tile, n), lambda i, info: (i, 0))
    return pl.pallas_call(
        functools.partial(out_proj_kernel, plan, len(pieces)),
        grid_spec=pltpu.PrefetchScalarGridSpec(
            num_scalar_prefetch=1,
            grid=(tok // tile,),
            in_specs=[ANY] * len(pieces)
            + [rows_of(width)]
            + [rows_of(feats)] * 4
            + [pl.BlockSpec((1, width), lambda i, info: (0, 0))],
            out_specs=[
                rows_of(width),
                rows_of(width),
                pl.BlockSpec((width, tile), lambda i, info: (0, i)),
                pl.BlockSpec((4, tile, feats), lambda i, info: (0, i, 0)),
            ],
            scratch_shapes=[pltpu.VMEM((4, width, feats), BF16), pltpu.SemaphoreType.DMA],
        ),
        out_shape=[
            shape_of((tok, width), F32),
            shape_of((tok, width), BF16),
            shape_of((width, tok), BF16),
            shape_of((4, tok, feats), BF16),
        ],
        compiler_params=settings(1, 60),
        cost_estimate=cost(True),
        name="out_proj",
    )(info, *pieces, x, *mine, *theirs, gain)


def norm_two_back_kernel(plan, count, info, *refs):
    g_ref, r_ref, gr_ref, gain_ref, gres_ref, gat_ref, a0, a1, b0, b1, gg_ref, w_ref, sem = refs[count:]
    load_blocks(plan, refs, w_ref, sem)
    ctx = info[2]
    grad, resid = g_ref[...], r_ref[...]
    rho = lax.rsqrt(jnp.mean(resid * resid, axis=-1, keepdims=True) + EPS)
    unit = resid * rho
    scaled = grad * gain_ref[...]
    back = rho * (scaled - unit * jnp.mean(scaled * unit, axis=-1, keepdims=True))
    total = gr_ref[...] + back
    gres_ref[...] = total
    low = total.astype(BF16)
    gat_ref[...] = total.T.astype(BF16)

    @pl.when(pl.program_id(0) == 0)
    def _():
        gg_ref[...] = jnp.zeros_like(gg_ref)

    gg_ref[...] += jnp.sum(grad * unit, axis=0, keepdims=True)
    for j, ref, side in ((0, a0, ctx), (1, a1, ctx), (0, b0, 1 - ctx), (1, b1, 1 - ctx)):
        ref[...] = dot(low, w_ref[2 * side + j], 1, 0).astype(BF16)


def norm_two_back(info, grad, resid, grad_result, gain, weights, tile):
    plan, pieces = weights
    tok, width = grad.shape
    feats = pieces[0].shape[1]
    rows_of = lambda n: pl.BlockSpec((tile, n), lambda i, info: (i, 0))
    row = pl.BlockSpec((1, width), lambda i, info: (0, 0))
    return pl.pallas_call(
        functools.partial(norm_two_back_kernel, plan, len(pieces)),
        grid_spec=pltpu.PrefetchScalarGridSpec(
            num_scalar_prefetch=1,
            grid=(tok // tile,),
            in_specs=[ANY] * len(pieces) + [rows_of(width)] * 3 + [row],
            out_specs=[rows_of(width), pl.BlockSpec((width, tile), lambda i, info: (0, i))]
            + [rows_of(feats)] * 4
            + [row],
            scratch_shapes=[pltpu.VMEM((4, width, feats), BF16), pltpu.SemaphoreType.DMA],
        ),
        out_shape=[shape_of((tok, width), F32), shape_of((width, tok), BF16)]
        + [shape_of((tok, feats), BF16)] * 4
        + [shape_of((1, width), F32)],
        compiler_params=settings(1, 60),
        cost_estimate=cost(True, 5.4),
        name="norm_two_back",
    )(info, *pieces, grad, resid, grad_result, gain)


def norm_one_back_kernel(plan, count, info, *refs):
    p0, p1, x_ref, gres_ref, gain_ref, out_ref, gg_ref, w_ref, sem = refs[count:]
    load_blocks(plan, refs, w_ref, sem)
    quarter = x_ref.shape[1] // 4
    grad = dot(p0[0], w_ref[0], 1, 1)
    grad = grad + dot(p1[0], w_ref[1], 1, 1)
    grad = grad + dot(p0[1], w_ref[2], 1, 1)
    grad = grad + dot(p1[1], w_ref[3], 1, 1)
    x = x_ref[...].astype(F32)
    rho = lax.rsqrt(jnp.mean(x * x, axis=-1, keepdims=True) + EPS)
    unit = x * rho
    scaled = grad * gain_ref[...]
    back = rho * (scaled - unit * jnp.mean(scaled * unit, axis=-1, keepdims=True))
    total = (gres_ref[...] + back).astype(BF16)
    for p, mask in enumerate(MASKS):
        at = pl.multiple_of(jnp.bitwise_xor(info[1], mask) * quarter, quarter)
        part = total[:, p * quarter : (p + 1) * quarter]

        out_ref[:, pl.ds(at, quarter)] = part

    @pl.when(pl.program_id(0) == 0)
    def _():
        gg_ref[...] = jnp.zeros_like(gg_ref)

    gg_ref[...] += jnp.sum(grad * unit, axis=0, keepdims=True)


def norm_one_back(info, pairs, weights, x, grad_resid, gain, tile, part):
    plan, pieces = weights
    tok, width = x.shape
    cols = pieces[0].shape[1]
    steps = tok // tile // 2
    first = part * steps
    rows_of = lambda n: pl.BlockSpec((tile, n), lambda i, info: (first + i, 0))
    out_rows = pl.BlockSpec((tile, width), lambda i, info: (i, 0))
    pair = pl.BlockSpec((2, tile, cols), lambda i, info: (0, first + i, 0))
    row = pl.BlockSpec((1, width), lambda i, info: (0, 0))
    return pl.pallas_call(
        functools.partial(norm_one_back_kernel, plan, len(pieces)),
        grid_spec=pltpu.PrefetchScalarGridSpec(
            num_scalar_prefetch=1,
            grid=(steps,),
            in_specs=[ANY] * len(pieces) + [pair, pair, rows_of(width), rows_of(width), row],
            out_specs=[out_rows, row],
            scratch_shapes=[pltpu.VMEM((4, width, cols), BF16), pltpu.SemaphoreType.DMA],
        ),
        out_shape=[shape_of((tok // 2, width), BF16), shape_of((1, width), F32)],
        compiler_params=settings(1, 60),
        cost_estimate=cost(True),
        name="norm_one_back",
    )(info, *pieces, *pairs, x, grad_resid, gain)


def weight_copies(plan, pieces, gate_up, down, gate_up_sem, down_sem):
    third = down.shape[1] // 3
    rows = down.shape[0] // 4
    wide, thin = [], []
    for p, chunks in enumerate(plan):
        block = pl.ds(p * rows, rows)
        for j, (piece, row, at) in enumerate(chunks):
            src = pieces[piece].at[pl.ds(row, rows)]
            wide.append(
                pltpu.make_async_copy(
                    src.at[:, pl.ds(at, 2 * third)],
                    gate_up.at[block, pl.ds(j * 2 * third, 2 * third)],
                    gate_up_sem,
                )
            )
            thin.append(
                pltpu.make_async_copy(
                    src.at[:, pl.ds(at + 2 * third, third)],
                    down.at[block, pl.ds(j * third, third)],
                    down_sem,
                )
            )
    return wide, thin


def split_act(act):
    third = act.shape[1] // 6
    part = lambda j: act[:, j * third : (j + 1) * third]
    return [(part(0), part(1)), (part(2), part(3)), (part(4), part(5))]


def ffn_fwd_kernel(tile, plans, last, info, scale, x_ref, in_ref, *rest):
    if last:
        teach_ref, rest = rest[0], rest[1:]
    pieces = []
    for plan in plans:
        count = 1 + max(place[0] for chunks in plan for place in chunks)
        pieces.append(rest[:count])
        rest = rest[count:]
    act_ref, hid_ref = rest[:2]
    if last:
        out_ref, gres_ref, low_ref, lowt_ref, sq_ref = rest[2:7]
        gate_up, down, total, sems = rest[7:]
    else:
        sum_ref, gate_up, down, total, sems = rest[2:]
    step, part = pl.program_id(0), pl.program_id(1)
    final = len(plans) - 1
    width = x_ref.shape[1]
    quarter = width // 4
    third = down.shape[2] // 3

    def copies(s):
        return weight_copies(
            plans[s], pieces[s], gate_up.at[s], down.at[s], sems.at[s, 0], sems.at[s, 1]
        )

    @pl.when((step == 0) & (part == 0))
    def _():
        for s in range(len(plans)):
            wide, thin = copies(s)
            for copy in wide + thin:
                copy.start()

    for s in range(len(plans)):

        @pl.when((step == s) & (part == 0))
        def _():
            pltpu.make_async_copy(gate_up.at[s], gate_up.at[s], sems.at[s, 0]).wait()

    rows = pl.ds(pl.multiple_of(part * tile, tile), tile)
    act = dot(x_ref[rows, :], gate_up[step], 1, 0)
    for j, (gate, upper) in enumerate(split_act(act)):
        sig = sigmoid(gate)
        silu = gate * sig
        hid_ref[0, :, j * third : (j + 1) * third] = (silu * upper).astype(BF16)
        at = 2 * j * third
        act_ref[0, :, at : at + third] = (upper * (sig + silu - silu * sig)).astype(BF16)
        act_ref[0, :, at + third : at + 2 * third] = silu.astype(BF16)
    for s in range(len(plans)):

        @pl.when((step == s) & (part == 0))
        def _():
            pltpu.make_async_copy(down.at[s], down.at[s], sems.at[s, 1]).wait()

    grown = dot(hid_ref[0], down[step], 1, 1)

    @pl.when(step == 0)
    def _():
        total[rows, :] = in_ref[...] + grown

    @pl.when(step > 0)
    def _():
        total[rows, :] += grown

    @pl.when(step == final)
    def _():
        result = total[rows, :]
        if not last:
            sum_ref[...] = result
            return
        tok = x_ref.shape[0]
        slot = info[2] * tok + part * tile + lax.broadcasted_iota(jnp.int32, (tile, 1), 0)
        valid = jnp.where(slot < info[3], 1.0, 0.0)
        square = jnp.zeros((tile, quarter), F32)
        for p, mask in enumerate(MASKS):
            at = pl.multiple_of(jnp.bitwise_xor(info[1], mask) * quarter, quarter)
            cols = slice(p * quarter, (p + 1) * quarter)
            value = result[:, cols]
            out_ref[:, pl.ds(at, quarter)] = value.astype(BF16)
            error = valid * (value - teach_ref[0, :, pl.ds(at, quarter)].astype(F32))
            square = square + error * error
            grad = error * scale[0]
            gres_ref[:, cols] = grad
            low_ref[:, cols] = grad.astype(BF16)
            lowt_ref[cols, :] = grad.T.astype(BF16)

        @pl.when(part == 0)
        def _():
            sq_ref[...] = jnp.zeros_like(sq_ref)

        sq_ref[...] += jnp.sum(square, axis=0, keepdims=True)


def ffn_fwd(info, scale, x, total, teacher, weights, units, tile):
    tok, width = x.shape
    pieces = [piece for _, group in weights for piece in group]
    count = len(weights)
    last = teacher is not None
    entry = lambda s, i: jnp.where(s == 0, i, tok // tile - 1)
    leave = lambda s, i: jnp.where(s == count - 1, i, 0)
    tiles = lambda n: pl.BlockSpec((tile, n), lambda s, i, info: (leave(s, i), 0))
    slab = lambda n: pl.BlockSpec((1, tile, n), lambda s, i, info: (s, i, 0))
    in_specs = [
        SMEM,
        whole((tok, width)),
        pl.BlockSpec((tile, width), lambda s, i, info: (entry(s, i), 0)),
    ]
    out_specs = [slab(2 * units), slab(units)]
    out_shape = [shape_of((count, tok, 2 * units), BF16), shape_of((count, tok, units), BF16)]
    if last:
        in_specs.append(
            pl.BlockSpec((1, tile, width), lambda s, i, info: (info[0], leave(s, i), 0))
        )
        out_specs += [
            tiles(width),
            tiles(width),
            tiles(width),
            pl.BlockSpec((width, tile), lambda s, i, info: (0, leave(s, i))),
            pl.BlockSpec((1, width // 4), lambda s, i, info: (0, 0)),
        ]
        out_shape += [
            shape_of((tok, width), BF16),
            shape_of((tok, width), F32),
            shape_of((tok, width), BF16),
            shape_of((width, tok), BF16),
            shape_of((1, width // 4), F32),
        ]
    else:
        out_specs.append(tiles(width))
        out_shape.append(shape_of((tok, width), F32))
    return pl.pallas_call(
        functools.partial(ffn_fwd_kernel, tile, [plan for plan, _ in weights], last),
        grid_spec=pltpu.PrefetchScalarGridSpec(
            num_scalar_prefetch=1,
            grid=(count, tok // tile),
            in_specs=in_specs + [ANY] * len(pieces),
            out_specs=out_specs,
            scratch_shapes=[
                pltpu.VMEM((count, width, 2 * units), BF16),
                pltpu.VMEM((count, width, units), BF16),
                pltpu.VMEM((tok, width), F32),
                pltpu.SemaphoreType.DMA((count, 2)),
            ],
        ),
        out_shape=out_shape,
        compiler_params=settings(2, 60),
        cost_estimate=cost(True),
        name="ffn_fwd",
    )(info, scale, x, total, *([teacher] if last else []), *pieces)


def ffn_bwd_kernel(steps, plan, first, low_ref, act_ref, hid_ref, xt_ref, lowt_ref, *rest):
    count = 1 + max(place[0] for chunks in plan for place in chunks)
    pieces, rest = rest[:count], rest[count:]
    if not first:
        in_ref, rest = rest[0], rest[1:]
    out_ref, keep_ref, send_ref, gate_up, down, dact_all, hid_all, sems = rest
    step = pl.program_id(0)
    units = down.shape[1]
    third = units // 3
    tile = low_ref.shape[0]

    @pl.when(step == 0)
    def _():
        wide, thin = weight_copies(plan, pieces, gate_up, down, sems.at[0], sems.at[1])
        for copy in thin + wide:
            copy.start()
        pltpu.make_async_copy(down, down, sems.at[1]).wait()

    @pl.when(step < steps)
    def _():
        rows = pl.ds(pl.multiple_of(step * tile, tile), tile)
        grad_hidden = dot(low_ref[...], down[...], 1, 0)
        for j, (to_gate, to_upper) in enumerate(split_act(act_ref[0])):
            grad = grad_hidden[:, j * third : (j + 1) * third]
            at = 2 * j * third
            dact_all[rows, at : at + third] = (grad * to_gate.astype(F32)).astype(BF16)
            dact_all[rows, at + third : at + 2 * third] = (grad * to_upper.astype(F32)).astype(BF16)
        hid_all[rows, :] = hid_ref[0]

        @pl.when(step == 0)
        def _():
            pltpu.make_async_copy(gate_up, gate_up, sems.at[0]).wait()

        grown = dot(dact_all[rows, :], gate_up[...], 1, 1)
        out_ref[...] = grown if first else in_ref[...] + grown

    def weight_rows(target):
        target[:, : 2 * units] = dot(xt_ref[...], dact_all[...], 1, 0).astype(BF16)
        target[:, 2 * units :] = dot(lowt_ref[...], hid_all[...], 1, 0).astype(BF16)

    @pl.when((step >= steps) & (step < steps + 2))
    def _():
        weight_rows(send_ref)

    @pl.when(step >= steps + 2)
    def _():
        weight_rows(keep_ref)


def ffn_bwd(low, saved, weights, total, xt, lowt, tile):
    plan, pieces = weights
    acts, hiddens, block = saved
    tok, width = low.shape
    units = hiddens.shape[2]
    steps = tok // tile
    quarter = width // 4
    first = total is None
    clip = lambda i: jnp.minimum(i, steps - 1)
    rows_of = lambda n: pl.BlockSpec((tile, n), lambda i: (clip(i), 0))
    slab = lambda n: pl.BlockSpec((1, tile, n), lambda i: (block, clip(i), 0))
    feature = lambda i: (jnp.where(i < steps + 2, jnp.maximum(i - steps, 0) + 2, i - steps - 2), 0)
    return pl.pallas_call(
        functools.partial(ffn_bwd_kernel, steps, plan, first),
        grid=(steps + 4,),
        in_specs=[
            rows_of(width),
            slab(2 * units),
            slab(units),
            pl.BlockSpec((quarter, tok), feature),
            pl.BlockSpec((quarter, tok), feature),
        ]
        + [ANY] * len(pieces)
        + ([] if first else [rows_of(width)]),
        out_specs=[
            rows_of(width),
            pl.BlockSpec((quarter, 3 * units), lambda i: (jnp.maximum(i - steps - 2, 0), 0)),
            pl.BlockSpec((quarter, 3 * units), lambda i: (jnp.clip(i - steps, 0, 1), 0)),
        ],
        out_shape=[
            shape_of((tok, width), F32),
            shape_of((width // 2, 3 * units), BF16),
            shape_of((width // 2, 3 * units), BF16),
        ],
        scratch_shapes=[
            pltpu.VMEM((width, 2 * units), BF16),
            pltpu.VMEM((width, units), BF16),
            pltpu.VMEM((tok, 2 * units), BF16),
            pltpu.VMEM((tok, units), BF16),
            pltpu.SemaphoreType.DMA((2,)),
        ],
        input_output_aliases={} if first else {5 + len(pieces): 0},
        compiler_params=settings(1, 60),
        cost_estimate=cost(True, 11.2),
        name="ffn_bwd",
    )(low, acts, hiddens, xt, lowt, *pieces, *([] if first else [total]))


def turn_chunks(block):
    wide = block.shape[1] * 2 // 9
    thin = wide // 2
    starts = [(2 * wide, wide), (wide, wide), (0, wide)]
    starts += [(3 * wide + 2 * thin, thin), (3 * wide + thin, thin), (3 * wide, thin)]
    return jnp.concatenate([block[:, a : a + n] for a, n in starts], axis=1)


def sum_kernel(turns, *refs):
    total = None
    for ref, turn in zip(refs[:-1], turns):
        value = ref[...].astype(F32)
        value = turn_chunks(value) if turn else value
        total = value if total is None else total + value
    refs[-1][...] = total.astype(refs[-1].dtype)


def summed(terms, turns=None, dtype=BF16):
    rows, cols = terms[0].shape
    spec = pl.BlockSpec((128, cols), lambda i: (i, 0))
    return pl.pallas_call(
        functools.partial(sum_kernel, turns or [False] * len(terms)),
        grid=(rows // 128,),
        in_specs=[spec] * len(terms),
        out_specs=spec,
        out_shape=shape_of((rows, cols), dtype),
        compiler_params=settings(1, 60),
        cost_estimate=cost(False),
        name="summed",
    )(*terms)


def sums_kernel(jobs, count, info, *refs):
    arrays, refs = refs[:count], refs[count:]
    outs, (term_buf, out_buf, term_sems, out_sems) = refs[: len(jobs)], refs[len(jobs) :]
    rows = term_buf.shape[1]
    copies = []
    for terms in jobs:
        group = []
        for array, base, pick, _ in terms:
            at = base
            if pick is not None:
                at = pl.multiple_of(base + jnp.bitwise_xor(info[2], pick) * rows, rows)
            i = len(copies) + len(group)
            src = arrays[array].at[pl.ds(at, rows)]
            group.append(pltpu.make_async_copy(src, term_buf.at[i], term_sems.at[i]))
            group[-1].start()
        copies += group
    first = 0
    stores = []
    for j, terms in enumerate(jobs):
        total = None
        for i, (_, _, _, turn) in enumerate(terms):
            copies[first + i].wait()
            value = term_buf[first + i].astype(F32)
            value = turn_chunks(value) if turn else value
            total = value if total is None else total + value
        first += len(terms)
        out_buf[j] = total.astype(BF16)
        stores.append(pltpu.make_async_copy(out_buf.at[j], outs[j], out_sems.at[j]))
        stores[-1].start()
    for store in stores:
        store.wait()


def sums(info, arrays, jobs):
    cols = arrays[0].shape[1]
    rows, terms = 128, sum(len(job) for job in jobs)
    return pl.pallas_call(
        functools.partial(sums_kernel, jobs, len(arrays)),
        grid_spec=pltpu.PrefetchScalarGridSpec(
            num_scalar_prefetch=1,
            grid=(1,),
            in_specs=[ANY] * len(arrays),
            out_specs=[ANY] * len(jobs),
            scratch_shapes=[
                pltpu.VMEM((terms, rows, cols), BF16),
                pltpu.VMEM((len(jobs), rows, cols), BF16),
                pltpu.SemaphoreType.DMA((terms,)),
                pltpu.SemaphoreType.DMA((len(jobs),)),
            ],
        ),
        out_shape=[shape_of((rows, cols), BF16)] * len(jobs),
        compiler_params=settings(1, 60),
        cost_estimate=cost(False),
        name="sums",
    )(info, *arrays)


def core_jobs(keep, came):
    return [[(a, far * 256, pick, False) for a in (keep, came)] for far in (0, 1) for pick in (0, 1)]


def core_sum_kernel(info, left_ref, right_ref, *outs):
    total = (left_ref[...].astype(F32) + right_ref[...].astype(F32)).astype(BF16)
    block = pl.program_id(1)
    place = block // 2 * 2 + jnp.bitwise_xor(block % 2, info[2])
    for i, out in enumerate(outs):

        @pl.when(place == i)
        def _():
            out[...] = total


def core_sum(info, keep, came):
    groups, rows, cols = keep.shape
    spec = pl.BlockSpec((1, rows // 4, cols), lambda g, i, info: (g, i, 0))
    return pl.pallas_call(
        core_sum_kernel,
        grid_spec=pltpu.PrefetchScalarGridSpec(
            num_scalar_prefetch=1,
            grid=(groups, 4),
            in_specs=[spec] * 2,
            out_specs=[pl.BlockSpec((1, rows // 4, cols), lambda g, i, info: (g, 0, 0))] * 4,
        ),
        out_shape=[shape_of((groups, rows // 4, cols), BF16)] * 4,
        compiler_params=settings(2, 24),
        cost_estimate=cost(False),
        name="core_sum",
    )(info, keep, came)


def weight_grad_kernel(nt_ref, back0_ref, back1_ref, gt_ref, att_ref, keep_ref, send_ref):
    cols = back0_ref.shape[2]
    part, block = pl.program_id(0), pl.program_id(1)

    def rows(target, back_ref):
        target[0, :, :cols] = dot(nt_ref[...], back_ref[0], 1, 0).astype(BF16)
        target[0, :, cols:] = dot(gt_ref[...], att_ref[0], 1, 0).astype(BF16)

    for j, back_ref in enumerate((back0_ref, back1_ref)):

        @pl.when((part == 0) & (block % 2 == j))
        def _():
            rows(send_ref, back_ref)

        @pl.when((part == 1) & (block % 2 == j))
        def _():
            rows(keep_ref, back_ref)


def weight_grad(normed_t, backs, grad_t, attended):
    width, tok = normed_t.shape
    cols, feats = backs[0].shape[2], attended.shape[2]
    half = pl.BlockSpec((width // 2, tok), lambda p, k: (1 - p, 0))
    side = pl.BlockSpec((1, tok, cols), lambda p, k: (k // 2, 0, 0))
    shape = (1, width // 2, cols + feats)
    return pl.pallas_call(
        weight_grad_kernel,
        grid=(2, 4),
        in_specs=[half, side, side, half, pl.BlockSpec((1, tok, feats), lambda p, k: (k, 0, 0))],
        out_specs=[
            pl.BlockSpec(shape, lambda p, k: (jnp.where(p == 0, 0, k), 0, 0)),
            pl.BlockSpec(shape, lambda p, k: (jnp.where(p == 0, k, 3), 0, 0)),
        ],
        out_shape=[shape_of((4, width // 2, cols + feats), BF16)] * 2,
        compiler_params=settings(2, 60),
        cost_estimate=cost(True),
        name="weight_grad",
    )(normed_t, *backs, grad_t, attended)


def copy_kernel(in_ref, out_ref):
    out_ref[...] = in_ref[...]


def copied(array):
    spec = pl.BlockSpec((1,) + array.shape[1:], lambda i: (i, 0, 0))
    return pl.pallas_call(
        copy_kernel,
        grid=(array.shape[0],),
        in_specs=[spec],
        out_specs=spec,
        out_shape=shape_of(array.shape, array.dtype),
        compiler_params=settings(1, 24),
        cost_estimate=cost(False),
        name="copied",
    )(array)


def after(value, *others):
    return lax.optimization_barrier((value,) + others)[0]


class Live:

    def update(self, **values):
        vars(self).update(values)


def per_device_rows(
    tokens,
    teacher,
    lengths,
    attn_gain,
    q_weight,
    k_weight,
    v_weight,
    q_gain,
    k_gain,
    o_weight,
    ffn_gain,
    gate_weight,
    up_weight,
    down_weight,
):
    z = lax.axis_index("tp")
    ctx = lax.axis_index("ctx")
    fsdp = lax.axis_index("fsdp")
    rows_dev, tok, width = tokens.shape
    quarter = width // 4
    hd = q_gain.shape[0] * 4
    q_cols, k_cols = q_weight.shape[1], k_weight.shape[1]
    proj = q_cols + 2 * k_cols
    heads = (q_cols // hd, k_cols // hd)
    units = gate_weight.shape[1]
    slots = rows_dev * 4 * tok * 2

    def x_swap(v):
        return lax.ppermute(v, "fsdp", X_SWAP)

    def core_swap(v):
        return lax.ppermute(v, "fsdp", CORE_SWAP)

    def y_swap(v):
        return lax.ppermute(v, "ctx", Y_SWAP)

    def z_up(v):
        return lax.ppermute(v, "tp", Z_UP)

    def z_far(v):
        return lax.ppermute(v, "tp", Z_FAR)

    def z_down(v):
        return lax.ppermute(v, "tp", Z_DOWN)

    def natural(v):
        v = jnp.concatenate([v[0:1], v[2:3], v[1:2], v[3:4]], axis=0)
        v = jnp.where(fsdp % 2 == 0, v, jnp.concatenate([v[1:2], v[0:1], v[3:4], v[2:3]], axis=0))
        return jnp.where(fsdp // 2 == 0, v, jnp.concatenate([v[2:4], v[0:2]], axis=0))

    v = Live()

    def sync():
        v.update(**lax.optimization_barrier(dict(vars(v))))

    length = lax.dynamic_slice_in_dim(lengths, z, 1, 0)
    info = jnp.concatenate([jnp.stack([z, fsdp, ctx]).astype(jnp.int32), length])
    w_proj = join(q_weight, k_weight, v_weight)
    proj_z = [z_up(w_proj), z_far(w_proj), z_down(w_proj)]
    proj_own = jnp.concatenate([w_proj, x_swap(w_proj)], axis=0)
    count_here = jnp.sum(lengths).astype(F32)[None]
    vector = jnp.concatenate([attn_gain, ffn_gain, q_gain, k_gain]).astype(F32)
    vector = jnp.concatenate([vector, count_here, jnp.zeros((640 - 545,), F32)])[None]
    vector = jnp.concatenate([vector, x_swap(vector)], axis=0)
    vector = jnp.concatenate([vector, core_swap(vector)], axis=0)
    w_out, w_ffn, *w_chunks = pack(info, o_weight, gate_weight, up_weight, down_weight)
    pos = (ctx * tok + jnp.arange(tok, dtype=jnp.int32)).astype(F32)
    frequency = THETA ** (-(2.0 * jnp.arange(hd // 2, dtype=F32)) / hd)
    angles = frequency[:, None] * pos[None, :]
    head_gains = natural(vector[:, 2 * quarter : 544])
    v.update(
        info=info,
        proj_own=proj_own,
        proj_z=jnp.concatenate(proj_z, axis=0),
        w_out=w_out,
        w_ffn=w_ffn,
        w_chunks=w_chunks,
        gain_one=vector[:, :quarter].reshape(1, width),
        gain_two=vector[:, quarter : 2 * quarter].reshape(1, width),
        total_count=jnp.sum(vector[:, 544]),
        gain_q=head_gains[:, : hd // 4].reshape(hd, 1),
        gain_k=head_gains[:, hd // 4 :].reshape(hd, 1),
        cos_part=jnp.cos(angles),
        sin_part=jnp.sin(angles),
    )
    sync()
    info = v.info

    proj_zfar = x_swap(v.proj_z)
    out_z = [z_up(v.w_out), z_far(v.w_out), z_down(v.w_out)]
    own_core = core_swap(v.proj_own)
    x_in, normed_one_t = norm_one(info, tokens, v.gain_one, 256)
    v.update(
        proj_zfar=proj_zfar, own_core=own_core, x_in=x_in, normed_one_t=normed_one_t, out_z=out_z
    )
    sync()

    plan_proj = [[(0, 0), (0, quarter), (3, 0), (3, quarter)]]
    plan_proj += [[(p, k * quarter) for p in (1, 2, 4, 5)] for k in range(3)]
    weights_proj = [v.proj_own, v.proj_z, v.proj_zfar, v.own_core]
    weights_proj += [core_swap(v.proj_z), core_swap(v.proj_zfar)]
    one = [z_up(v.w_chunks[0]), z_up(v.w_chunks[3])]
    ffn_far = x_swap(v.w_ffn)
    tables = [v.cos_part, v.sin_part, v.gain_q, v.gain_k]

    def make(block, *then):
        normed_t = after(v.normed_one_t, *then)
        return project(info, (plan_proj, weights_proj), normed_t, *tables, heads, block)

    theirs = [make(lambda s: 2 * (1 - s[2]))]
    got = [y_swap(theirs[0][0])]
    theirs.append(make(lambda s: 2 * (1 - s[2]) + 1, theirs[0][0]))
    got.append(y_swap(theirs[1][0]))
    mine = [make(lambda s: 2 * s[2], theirs[1][0])]
    mine.append(make(lambda s: 2 * s[2] + 1, mine[0][0]))
    v.update(
        one=one,
        ffn_far=ffn_far,
        weights_proj=weights_proj,
        mine=mine,
        theirs=theirs,
        got0=got[0],
    )
    sync()

    one_far = [x_swap(v.one[0])]
    three = [z_down(v.w_chunks[0])]
    own_cores = [core_swap(v.w_ffn), core_swap(v.ffn_far)]
    first = attn_fwd(info, v.mine[0][0], v.got0, hd)
    v.update(first=first, got1=got[1], one_far=one_far, three=three, own_cores=own_cores)
    sync()

    arrived = [y_swap(v.first[1])]
    three = v.three + [z_down(v.w_chunks[1])]
    out_blocks = jnp.concatenate([v.w_out] + v.out_z, axis=0)
    out_far = x_swap(out_blocks)
    one_cores = [core_swap(v.one[0]), core_swap(v.one_far[0])]
    second = attn_fwd(info, v.mine[1][0], v.got1, hd)
    v.update(
        second=second,
        arrived=arrived,
        three=three,
        out_blocks=out_blocks,
        out_far=out_far,
        one_cores=one_cores,
    )
    sync()

    arrived = v.arrived + [y_swap(v.second[1])]
    three = v.three + [z_down(v.w_chunks[2])]
    one_far = v.one_far + [x_swap(v.one[1][:, :units])]
    weights_out = [v.out_blocks, v.out_far]
    weights_out += [core_swap(v.out_blocks), core_swap(v.out_far)]
    v.update(arrived=arrived, three=three, one_far=one_far, weights_out=weights_out)
    sync()

    plan_out = [[(p, k * quarter) for p in range(4)] for k in range(4)]
    two = [z_up(v.one[0])]
    three_far = [x_swap(v.three[0])]
    one_far = v.one_far + [y_swap(v.one_far[0])]
    one_cores = v.one_cores + [core_swap(v.one[1]), core_swap(v.one_far[1])]
    resid, normed_two, normed_two_t, attended = out_proj(
        info,
        v.x_in,
        [v.first[0], v.second[0]],
        v.arrived,
        (plan_out, v.weights_out),
        v.gain_two,
        256,
    )
    v.update(
        two=two,
        three_far=three_far,
        one_far=one_far,
        one_cores=one_cores,
        resid=resid,
        normed_two=normed_two,
        normed_two_t=normed_two_t,
        attended=attended,
    )
    sync()

    plan0 = [[(i, 0, j * units) for j in range(3)] for i in range(4)]
    plan_mixed = [[(0, 0, 0), (1, 0, 0), (1, 0, units)], [(i, 0, 0) for i in (2, 3, 4)]]
    plan_mixed += [[(5, 0, 0), (6, 0, 0), (6, 0, units)], [(i, 0, 0) for i in (7, 8, 9)]]
    scale = (slots / v.total_count)[None]
    weights0 = [v.w_ffn, v.ffn_far] + v.own_cores
    c0, cf, c1, cb = v.one_cores
    weights1 = v.one + v.one_far + [c0, c1, cf, cb, core_swap(v.one_far[2])]
    two = v.two + [z_up(v.one[1])]
    three_far = v.three_far + [x_swap(v.three[1]), y_swap(v.three_far[0])]
    two_far = [x_swap(v.two[0])]
    three_cores = [core_swap(v.three[0])]
    acts_a, hiddens_a, sum_a = ffn_fwd(
        info,
        scale,
        v.normed_two,
        v.resid,
        None,
        [(plan0, weights0), (plan_mixed, weights1)],
        units,
        256,
    )
    v.update(
        scale=scale,
        weights0=weights0,
        weights1=weights1,
        two=two,
        three_far=three_far,
        two_far=two_far,
        three_cores=three_cores,
        acts_a=acts_a,
        hiddens_a=hiddens_a,
        sum_a=sum_a,
    )
    sync()

    plan_chunks = [[(3 * p + j, 0, 0) for j in range(3)] for p in range(4)]
    weights3 = v.three + v.three_far + v.three_cores
    weights3 += [core_swap(part) for part in v.three[1:]]
    weights3 += [core_swap(part) for part in v.three_far]
    two_far = v.two_far + [x_swap(v.two[1][:, :units]), y_swap(v.two_far[0])]
    two_cores = [core_swap(part) for part in v.two + v.two_far]
    acts_b, hiddens_b, sum_b = ffn_fwd(
        info, v.scale, v.normed_two, v.sum_a, None, [(plan_chunks, weights3)], units, 256
    )
    v.update(
        weights3=weights3,
        two_far=two_far,
        two_cores=two_cores,
        acts_b=acts_b,
        hiddens_b=hiddens_b,
        sum_b=sum_b,
    )
    sync()

    weights2 = v.two + v.two_far + v.two_cores
    weights2 += [core_swap(part) for part in v.two_far[1:]]
    acts_c, hiddens_c, result_low, grad_result, grad_low, grad_low_t, square = ffn_fwd(
        info, v.scale, v.normed_two, v.sum_b, teacher, [(plan_mixed, weights2)], units, 256
    )
    v.update(
        weights2=weights2,
        acts_c=acts_c,
        hiddens_c=hiddens_c,
        result_low=result_low,
        grad_result=grad_result,
        grad_low=grad_low,
        grad_low_t=grad_low_t,
        square=square,
    )
    sync()

    def ffn_back(plan, weights, acts, hiddens, block, total):
        return ffn_bwd(
            v.grad_low,
            (acts, hiddens, block),
            (plan, weights),
            total,
            v.normed_two_t,
            v.grad_low_t,
            256,
        )

    turned = [False, False, True]
    output = lax.all_gather(v.result_low, "tp", axis=0, tiled=False)
    total, keep2, send2 = ffn_back(plan_mixed, v.weights2, v.acts_c, v.hiddens_c, 0, None)
    v.update(total=total, keep2=keep2, send2=send2)
    sync()

    came2 = core_swap(v.send2)
    total, keep1, send1 = ffn_back(plan_mixed, v.weights1, v.acts_a, v.hiddens_a, 1, v.total)
    v.update(came2=came2, total=total, keep1=keep1, send1=send1)
    sync()

    came1 = core_swap(v.send1)
    sum2 = sums(info, [v.keep2, v.came2], core_jobs(0, 1))
    far_t2 = x_swap(sum2[3])
    total, keep3, send3 = ffn_back(
        plan_chunks, v.weights3, v.acts_b, v.hiddens_b, 0, after(v.total, sum2[0])
    )
    v.update(
        came1=came1,
        sum2=sum2,
        far_t2=far_t2,
        total=total,
        keep3=keep3,
        send3=send3,
    )
    sync()

    came3 = core_swap(v.send3)
    far_h2 = x_swap(v.sum2[2])
    there2, *sum1 = sums(
        info,
        [v.sum2[1], v.far_t2, v.keep1, v.came1],
        [[(0, 0, None, False), (1, 0, None, False)]] + core_jobs(2, 3),
    )
    there2 = y_swap(there2)
    total, keep0, send0 = ffn_back(
        plan0, v.weights0, v.acts_a, v.hiddens_a, 0, after(v.total, sum1[0])
    )
    v.update(
        came3=came3,
        far_h2=far_h2,
        there2=there2,
        sum1=sum1,
        total=total,
        keep0=keep0,
        send0=send0,
    )
    sync()

    came0 = core_swap(v.send0)
    far_t1 = x_swap(v.sum1[3])
    plane = [(0, 0, None, False), (1, 0, None, False), (2, 0, None, True)]
    part2, *sum3 = sums(
        info,
        [v.sum2[0], v.far_h2, v.there2, v.keep3, v.came3],
        [plane] + core_jobs(3, 4),
    )
    down2 = z_down(part2)
    grad_resid, grad_attn_t, a0, a1, b0, b1, gain_two_sum = norm_two_back(
        info,
        after(v.total, sum3[0]),
        v.resid,
        v.grad_result,
        v.gain_two,
        (plan_out, v.weights_out),
        256,
    )
    grad_got = [y_swap(b0), y_swap(b1)]
    v.update(
        came0=came0,
        far_t1=far_t1,
        sum3=sum3,
        grad_resid=grad_resid,
        grad_attn_t=grad_attn_t,
        grad_mine=[a0, a1],
        gain_two_sum=gain_two_sum,
    )
    sync()

    def attn_back(j, grad):
        out = (v.first, v.second)[j]
        got_ref = (v.got0, v.got1)[j]
        arrived = (v.grad_got0, grad_got[1] if j == 0 else v.grad_got1)[j]
        return attn_bwd(
            info, v.mine[j][0], got_ref, out[0], out[1], grad, arrived, out[2], hd
        )

    far_h1 = x_swap(v.sum1[2])
    there1, *sum0 = sums(
        info,
        [v.sum1[1], v.far_t1, v.keep0, v.came0],
        [[(0, 0, None, False), (1, 0, None, False)]] + core_jobs(2, 3),
    )
    there1 = y_swap(there1)
    far_t3 = x_swap(v.sum3[3])
    v.update(grad_got0=grad_got[0])
    back0 = attn_back(0, after(v.grad_mine[0], sum0[0]))
    v.update(
        far_h1=far_h1,
        there1=there1,
        far_t3=far_t3,
        down2=down2,
        sum0=sum0,
        back0=back0,
        grad_got1=grad_got[1],
    )
    sync()

    heads0 = y_swap(v.back0[1])
    far_h3 = x_swap(v.sum3[2])
    far_t0 = x_swap(v.sum0[3])
    there3, two_down = sums(
        info,
        [v.sum3[1], v.far_t3, v.sum1[0], v.far_h1, v.there1, v.down2],
        [
            [(0, 0, None, False), (1, 0, None, False)],
            [(2, 0, None, False), (3, 0, None, False), (4, 0, None, True), (5, 0, None, False)],
        ],
    )
    there3_got = y_swap(there3)
    two_down_got = z_down(two_down)
    back1 = attn_back(1, after(v.grad_mine[1], there3, two_down, output))
    v.update(
        heads0=heads0, far_h3=far_h3, far_t0=far_t0, there3=there3_got, back1=back1
    )
    sync()

    heads1 = y_swap(v.back1[1])
    far_h0 = x_swap(v.sum0[2])
    part3, there0 = sums(
        info,
        [v.sum3[0], v.far_h3, v.there3, v.sum0[1], v.far_t0],
        [plane, [(3, 0, None, False), (4, 0, None, False)]],
    )
    up3 = z_up(part3)
    tables = [v.cos_part, v.sin_part, v.gain_q, v.gain_k]
    head0 = head_back(
        info, v.back0[0], v.heads0, v.mine[0][1], v.theirs[0][1], *tables, heads
    )
    v.update(heads1=heads1, head0=head0, there0=there0)
    sync()

    there0 = y_swap(v.there0)
    head1 = head_back(
        info, v.back1[0], v.heads1, v.mine[1][1], v.theirs[1][1], *tables, heads
    )
    def last_norm(part, *then):
        return norm_one_back(
            info,
            [v.head0[0], after(head1[0], *then)],
            (plan_proj, v.weights_proj),
            v.x_in,
            v.grad_resid,
            v.gain_one,
            tok // 4,
            part,
        )

    low_first, gain_first = last_norm(0)
    low_second, gain_second = last_norm(1, low_first)
    gathered = [lax.all_gather(low_first, "tp", axis=0, tiled=False)]
    tokens_low, gain_one_sum = low_second, gain_first + gain_second
    v.update(head1=head1, tokens_low=tokens_low, gain_one_sum=gain_one_sum, up3=up3)
    v.update(there0=there0, far_h0=far_h0, two_down=two_down_got)
    sync()

    gathered.append(lax.all_gather(v.tokens_low, "tp", axis=0, tiled=False))
    keep, send = weight_grad(
        v.normed_one_t, [v.head0[0], v.head1[0]], v.grad_attn_t, v.attended
    )
    gain_heads = v.head0[1] + v.head1[1]
    vector = jnp.concatenate(
        [
            natural(v.gain_one_sum.reshape(4, quarter)).reshape(1, width),
            natural(v.gain_two_sum.reshape(4, quarter)).reshape(1, width),
            gain_heads[:, 0].reshape(1, hd),
            gain_heads[:, 1].reshape(1, hd),
            jnp.sum(v.square).reshape(1, 1),
            jnp.zeros((1, 127), F32),
        ],
        axis=1,
    )
    vector = vector + core_swap(vector)
    v.update(keep=keep, send=send)
    v.update(vector=vector)
    sync()

    rows = quarter // 2
    flat = lambda a: a.reshape(4 * rows, a.shape[-1])
    attn_sums = [flat(p) for p in core_sum(info, v.keep, core_swap(v.send))]
    vector = v.vector + x_swap(v.vector)
    v.update(sums=attn_sums, vector=vector)
    sync()

    far_t = x_swap(v.sums[3])
    part0 = summed([v.sum0[0], v.far_h0, v.there0], turned)
    ffn_sum = summed([part0, v.two_down, v.up3], None, F32)
    vector = v.vector + y_swap(v.vector)
    v.update(far_t=far_t, ffn_sum=ffn_sum, vector=vector)
    sync()

    far_h = x_swap(v.sums[2])
    there = y_swap(summed([v.sums[1], v.far_t]))
    spread = copied(output)
    v.update(far_h=far_h, there=there, spread=spread)
    sync()

    parts = summed([v.sums[0], v.far_h, v.there])
    parts = [parts[k * rows : (k + 1) * rows] for k in range(4)]
    parts = [parts[0], z_down(parts[1]), z_far(parts[2]), z_up(parts[3])]
    ffn_other = y_swap(v.ffn_sum)
    v.update(parts=parts)
    sync()

    attn_sum = summed(v.parts, None, F32)
    vector = v.vector + lax.ppermute(v.vector, "tp", Z_NEAR)
    v.update(attn_sum=attn_sum, vector=vector)
    v.update(ffn_other=ffn_other)
    sync()

    def finish(own, other):
        return jnp.concatenate(
            [jnp.where(ctx == 0, own, other), jnp.where(ctx == 0, other, own)], axis=0
        )

    def columns(first):
        parts = [ffn_grad[:, first(j) : first(j) + third] for j in range(3)]
        return jnp.concatenate(
            [
                jnp.where(ctx == 0, parts[0], parts[2]),
                parts[1],
                jnp.where(ctx == 0, parts[2], parts[0]),
            ],
            axis=1,
        )

    attn_other = y_swap(v.attn_sum)
    vector = v.vector + lax.ppermute(v.vector, "tp", Z_FAR)
    third = units // 3
    ffn_grad = finish(v.ffn_sum, turn_chunks(v.ffn_other))
    grad_gate = columns(lambda j: 2 * j * third)
    grad_up = columns(lambda j: (2 * j + 1) * third)
    grad_down = columns(lambda j: 2 * units + j * third).T
    grad = jnp.zeros((rows_dev, tok, width), F32)
    grad = lax.dynamic_update_slice(grad, gathered[0].astype(F32), (0, 0, 0))
    v.update(vector=vector, attn_other=attn_other, grad=grad)
    v.update(grad_gate=grad_gate, grad_up=grad_up, grad_down=grad_down)
    sync()

    tokens_grad = lax.dynamic_update_slice(v.grad, gathered[1].astype(F32), (0, tok // 2, 0))
    sums_all = v.vector[0]

    attn_grad = finish(v.attn_sum, v.attn_other)
    teacher_loss = sums_all[2 * width + 2 * hd] / (v.total_count * width)

    def own_part(at, size):
        return lax.dynamic_slice_in_dim(sums_all, at + fsdp * (size // 4), size // 4, 0)

    return (
        v.spread,
        teacher_loss,
        tokens_grad,
        own_part(0, width),
        attn_grad[:, :q_cols],
        attn_grad[:, q_cols : q_cols + k_cols],
        attn_grad[:, q_cols + k_cols : proj],
        own_part(2 * width, hd),
        own_part(2 * width + hd, hd),
        attn_grad[:, proj:].T,
        own_part(width, width),
        v.grad_gate,
        v.grad_up,
        v.grad_down,
    )


def solution(mesh):
    return jax.shard_map(
        per_device_rows if fits(mesh) else per_device_any,
        mesh=mesh,
        in_specs=(
            P("fsdp", "ctx", None),
            P("fsdp", "ctx", None),
            P("fsdp"),
            P("fsdp"),
            P("fsdp", "tp"),
            P("fsdp", "tp"),
            P("fsdp", "tp"),
            P("fsdp"),
            P("fsdp"),
            P("tp", "fsdp"),
            P("fsdp"),
            P("fsdp", "tp"),
            P("fsdp", "tp"),
            P("tp", "fsdp"),
        ),
        out_specs=(
            P("fsdp", "ctx", None),
            P(),
            P("fsdp", "ctx", None),
            P("fsdp"),
            P("fsdp", "tp"),
            P("fsdp", "tp"),
            P("fsdp", "tp"),
            P("fsdp"),
            P("fsdp"),
            P("tp", "fsdp"),
            P("fsdp"),
            P("fsdp", "tp"),
            P("fsdp", "tp"),
            P("tp", "fsdp"),
        ),
        check_vma=False,
    )
```

```python
import functools
import math

import jax
import jax.numpy as jnp
from jax import lax
from jax.experimental import pallas as pl
from jax.experimental.pallas import tpu as pltpu
from jax.sharding import PartitionSpec as P

EPS = 1e-05
THETA = 1000000.0
NEGATIVE = -1e30


def rms_scale(field_in, gain_vec):
    return (
        field_in * lax.rsqrt(jnp.mean(field_in * field_in, axis=-1, keepdims=True) + EPS) * gain_vec
    )


def rotate(field_in, positions):
    half_dim = field_in.shape[-1] // 2
    frequency = THETA ** (-(2.0 * jnp.arange(half_dim, dtype=jnp.float32)) / field_in.shape[-1])
    angles = positions[:, None] * frequency[None, :]
    cos_part = jnp.cos(angles)[:, None, :]
    sin_part = jnp.sin(angles)[:, None, :]
    lower_half = field_in[..., :half_dim]
    upper_half = field_in[..., half_dim:]
    return jnp.concatenate(
        [
            lower_half * cos_part - upper_half * sin_part,
            upper_half * cos_part + lower_half * sin_part,
        ],
        axis=-1,
    )


def linear(left_mat, right_mat):
    return jnp.dot(left_mat, right_mat, preferred_element_type=jnp.float32)


def linear_left(left_mat, right_mat):
    return lax.dot_general(
        left_mat, right_mat, (((0,), (0,)), ((), ())), preferred_element_type=jnp.float32
    )


def linear_right(left_mat, right_mat):
    return lax.dot_general(
        left_mat, right_mat, (((1,), (1,)), ((), ())), preferred_element_type=jnp.float32
    )


def swiglu(gate_act, up_act):
    return jax.nn.silu(gate_act) * up_act


def per_device_any(
    tokens,
    teacher,
    lengths,
    attn_gain,
    q_weight,
    k_weight,
    v_weight,
    q_gain,
    k_gain,
    o_weight,
    ffn_gain,
    gate_weight,
    up_weight,
    down_weight,
):
    (
        gain_one,
        w_query,
        w_key,
        w_value,
        gain_query,
        gain_key,
        w_output,
        gain_two,
        w_gate,
        w_upper,
        w_down,
    ) = (
        lax.all_gather(attn_gain, "fsdp", axis=0, tiled=True),
        lax.all_gather(q_weight, "fsdp", axis=0, tiled=True),
        lax.all_gather(k_weight, "fsdp", axis=0, tiled=True),
        lax.all_gather(v_weight, "fsdp", axis=0, tiled=True),
        lax.all_gather(q_gain, "fsdp", axis=0, tiled=True),
        lax.all_gather(k_gain, "fsdp", axis=0, tiled=True),
        lax.all_gather(o_weight, "fsdp", axis=1, tiled=True),
        lax.all_gather(ffn_gain, "fsdp", axis=0, tiled=True),
        lax.all_gather(gate_weight, "fsdp", axis=0, tiled=True),
        lax.all_gather(up_weight, "fsdp", axis=0, tiled=True),
        lax.all_gather(down_weight, "fsdp", axis=1, tiled=True),
    )
    rows_dev, block_len, model_width = tokens.shape
    count_tok = rows_dev * block_len
    head_dim = gain_query.shape[0]
    q_heads = w_query.shape[1] // head_dim
    kv_heads = w_key.shape[1] // head_dim
    group_size = q_heads // kv_heads
    score_scale = head_dim ** (-0.5)
    row_len = block_len * lax.axis_size("ctx")
    key_block = math.gcd(row_len, 512)
    block_start = lax.axis_index("ctx") * block_len
    tiles_used = (block_start + block_len + key_block - 1) // key_block
    slot_pos = block_start + jnp.arange(block_len, dtype=jnp.int32)
    positions = slot_pos.astype(jnp.float32)
    valid = (slot_pos[None, :] < lengths[:, None]).astype(jnp.float32)
    slots = count_tok * lax.axis_size("fsdp") * lax.axis_size("ctx")
    gain_two_f = gain_two.astype(jnp.float32)
    gain_one_f = gain_one.astype(jnp.float32)
    inputs = tokens.astype(jnp.float32)
    normed_one, back_one = jax.vjp(rms_scale, inputs, gain_one_f)
    normed_low = normed_one.astype(jnp.bfloat16).reshape(count_tok, model_width)
    query_raw = linear(normed_low, w_query)
    key_raw = linear(normed_low, w_key)
    value_raw = linear(normed_low, w_value)

    def heads_post(raw_heads, gain_vec):
        shaped = raw_heads.reshape(rows_dev, block_len, -1, head_dim)
        return rotate(rms_scale(shaped, gain_vec), positions)

    query_rot, query_back = jax.vjp(heads_post, query_raw, gain_query.astype(jnp.float32))
    key_rot, key_back = jax.vjp(heads_post, key_raw, gain_key.astype(jnp.float32))
    queries = query_rot.astype(jnp.bfloat16).reshape(
        rows_dev, block_len, kv_heads, group_size, head_dim
    )
    key_rows = key_rot.astype(jnp.bfloat16).reshape(rows_dev, block_len, kv_heads * head_dim)
    values = value_raw.astype(jnp.bfloat16).reshape(rows_dev, block_len, kv_heads * head_dim)
    keys_all, values_all = (
        lax.all_gather(key_rows, "ctx", axis=1, tiled=True),
        lax.all_gather(values, "ctx", axis=1, tiled=True),
    )

    def key_tile(tile_index):
        tile_start = tile_index * key_block
        key_pos = tile_start + jnp.arange(key_block, dtype=jnp.int32)
        key_part = lax.dynamic_slice_in_dim(keys_all, tile_start, key_block, 1).reshape(
            rows_dev, key_block, kv_heads, head_dim
        )
        value_part = lax.dynamic_slice_in_dim(values_all, tile_start, key_block, 1).reshape(
            rows_dev, key_block, kv_heads, head_dim
        )
        scores = (
            jnp.einsum("rqhgd,rkhd->rhgqk", queries, key_part, preferred_element_type=jnp.float32)
            * score_scale
        )
        allowed = (key_pos[None, None, :] <= slot_pos[None, :, None]) & (
            key_pos[None, None, :] < lengths[:, None, None]
        )
        return (tile_start, scores, allowed[:, None, None], key_part, value_part)

    stat_shape = (rows_dev, kv_heads, group_size, block_len)

    def stats_step(tile_index, carried):
        running_max, running_sum = carried
        tile_start, scores, allowed, key_part, value_part = key_tile(tile_index)
        masked = jnp.where(allowed, scores, NEGATIVE)
        new_max = jnp.maximum(running_max, jnp.max(masked, axis=-1))
        terms = jnp.where(allowed, jnp.exp(masked - new_max[..., None]), 0.0)
        return (new_max, running_sum * jnp.exp(running_max - new_max) + jnp.sum(terms, axis=-1))

    running_max, running_sum = lax.fori_loop(
        0,
        tiles_used,
        stats_step,
        (jnp.full(stat_shape, NEGATIVE, jnp.float32), jnp.zeros(stat_shape, jnp.float32)),
    )
    log_total = running_max + jnp.log(running_sum)
    out_shape = (rows_dev, block_len, kv_heads, group_size, head_dim)

    def value_step(tile_index, carried):
        rounded_out, exact_out = carried
        tile_start, scores, allowed, key_part, value_part = key_tile(tile_index)
        tile_probs = jnp.where(allowed, jnp.exp(scores - log_total[..., None]), 0.0)
        rounded_out = rounded_out + jnp.einsum(
            "rhgqk,rkhd->rqhgd",
            tile_probs.astype(jnp.bfloat16),
            value_part,
            preferred_element_type=jnp.float32,
        )
        exact_out = exact_out + jnp.einsum(
            "rhgqk,rkhd->rqhgd", tile_probs, value_part.astype(jnp.float32)
        )
        return (rounded_out, exact_out)

    rounded_out, exact_out = lax.fori_loop(
        0,
        tiles_used,
        value_step,
        (jnp.zeros(out_shape, jnp.float32), jnp.zeros(out_shape, jnp.float32)),
    )
    attended = rounded_out.astype(jnp.bfloat16).reshape(count_tok, q_heads * head_dim)
    attn_total = lax.psum(linear(attended, w_output), "tp")
    resid = inputs + attn_total.reshape(rows_dev, block_len, model_width)
    normed_two, back_two = jax.vjp(rms_scale, resid, gain_two_f)
    normed_second = normed_two.astype(jnp.bfloat16).reshape(count_tok, model_width)
    gate_act = linear(normed_second, w_gate)
    up_act = linear(normed_second, w_upper)
    hidden_full, back_glu = jax.vjp(swiglu, gate_act, up_act)
    hidden = hidden_full.astype(jnp.bfloat16)
    ffn_total = lax.psum(linear(hidden, w_down), "tp")
    result = resid + ffn_total.reshape(rows_dev, block_len, model_width)
    error_value = result - teacher.astype(jnp.float32)
    valid_col = valid[..., None]
    total_square, total_count = lax.psum(
        (jnp.sum(valid_col * error_value * error_value), jnp.sum(valid)), ("fsdp", "ctx")
    )
    teacher_loss = total_square / (total_count * model_width)
    grad_result = valid_col * error_value * (slots / total_count)
    grad_low = grad_result.astype(jnp.bfloat16).reshape(count_tok, model_width)
    grad_down = linear_left(hidden, grad_low)
    grad_hidden = linear_right(grad_low, w_down)
    grad_gate_full, grad_up_full = back_glu(grad_hidden)
    grad_gate = grad_gate_full.astype(jnp.bfloat16)
    grad_up = grad_up_full.astype(jnp.bfloat16)
    grad_wgate = linear_left(normed_second, grad_gate)
    grad_wup = linear_left(normed_second, grad_up)
    normed_two_part = linear_right(grad_gate, w_gate) + linear_right(grad_up, w_upper)
    grad_normed_two = lax.psum(normed_two_part, "tp")
    grad_resid_norm, grad_gain_two = back_two(
        grad_normed_two.reshape(rows_dev, block_len, model_width)
    )
    grad_resid = grad_result + grad_resid_norm
    grad_attn_low = grad_resid.astype(jnp.bfloat16).reshape(count_tok, model_width)
    grad_woutput = linear_left(attended, grad_attn_low)
    grad_attended = linear_right(grad_attn_low, w_output).astype(jnp.bfloat16).reshape(out_shape)
    delta = jnp.einsum("rqhgd,rqhgd->rhgq", grad_attended.astype(jnp.float32), exact_out)
    full_shape = (rows_dev, row_len, kv_heads * head_dim)

    def grad_step(tile_index, carried):
        grad_queries, grad_keys, grad_values = carried
        tile_start, scores, allowed, key_part, value_part = key_tile(tile_index)
        tile_probs = jnp.where(allowed, jnp.exp(scores - log_total[..., None]), 0.0)
        grad_probs = jnp.einsum(
            "rqhgd,rkhd->rhgqk", grad_attended, value_part, preferred_element_type=jnp.float32
        )
        grad_scores = (tile_probs * (grad_probs - delta[..., None])).astype(jnp.bfloat16)
        grad_queries = (
            grad_queries
            + jnp.einsum(
                "rhgqk,rkhd->rqhgd", grad_scores, key_part, preferred_element_type=jnp.float32
            )
            * score_scale
        )
        key_term = (
            jnp.einsum(
                "rhgqk,rqhgd->rkhd", grad_scores, queries, preferred_element_type=jnp.float32
            )
            * score_scale
        )
        value_term = jnp.einsum(
            "rhgqk,rqhgd->rkhd",
            tile_probs.astype(jnp.bfloat16),
            grad_attended,
            preferred_element_type=jnp.float32,
        )
        grad_keys = lax.dynamic_update_slice_in_dim(
            grad_keys, key_term.reshape(rows_dev, key_block, kv_heads * head_dim), tile_start, 1
        )
        grad_values = lax.dynamic_update_slice_in_dim(
            grad_values, value_term.reshape(rows_dev, key_block, kv_heads * head_dim), tile_start, 1
        )
        return (grad_queries, grad_keys, grad_values)

    grad_queries, grad_keys, grad_values = lax.fori_loop(
        0,
        tiles_used,
        grad_step,
        (
            jnp.zeros(out_shape, jnp.float32),
            jnp.zeros(full_shape, jnp.float32),
            jnp.zeros(full_shape, jnp.float32),
        ),
    )
    key_grad, value_grad = (
        lax.psum_scatter(grad_keys, "ctx", scatter_dimension=1, tiled=True),
        lax.psum_scatter(grad_values, "ctx", scatter_dimension=1, tiled=True),
    )
    grad_query_raw, grad_gain_query = query_back(
        grad_queries.reshape(rows_dev, block_len, q_heads, head_dim)
    )
    grad_key_raw, grad_gain_key = key_back(
        key_grad.reshape(rows_dev, block_len, kv_heads, head_dim)
    )
    query_low = grad_query_raw.astype(jnp.bfloat16)
    key_low = grad_key_raw.astype(jnp.bfloat16)
    value_low = value_grad.reshape(count_tok, kv_heads * head_dim).astype(jnp.bfloat16)
    grad_wquery = linear_left(normed_low, query_low)
    grad_wkey = linear_left(normed_low, key_low)
    grad_wvalue = linear_left(normed_low, value_low)
    normed_part = (
        linear_right(query_low, w_query)
        + linear_right(key_low, w_key)
        + linear_right(value_low, w_value)
    )
    grad_normed_one, grad_gain_query, grad_gain_key = lax.psum(
        (normed_part, grad_gain_query, grad_gain_key), "tp"
    )
    grad_input_norm, grad_gain_one = back_one(
        grad_normed_one.reshape(rows_dev, block_len, model_width)
    )
    tokens_grad = grad_resid + grad_input_norm
    partials = (
        grad_gain_one,
        grad_wquery,
        grad_wkey,
        grad_wvalue,
        grad_gain_query,
        grad_gain_key,
        grad_woutput,
        grad_gain_two,
        grad_wgate,
        grad_wup,
        grad_down,
    )
    pieces = (
        lax.psum_scatter(partials[0], ("fsdp", "ctx"), scatter_dimension=0, tiled=True),
        lax.psum_scatter(partials[1], ("fsdp", "ctx"), scatter_dimension=0, tiled=True),
        lax.psum_scatter(partials[2], ("fsdp", "ctx"), scatter_dimension=0, tiled=True),
        lax.psum_scatter(partials[3], ("fsdp", "ctx"), scatter_dimension=0, tiled=True),
        lax.psum_scatter(partials[4], ("fsdp", "ctx"), scatter_dimension=0, tiled=True),
        lax.psum_scatter(partials[5], ("fsdp", "ctx"), scatter_dimension=0, tiled=True),
        lax.psum_scatter(partials[6], ("fsdp", "ctx"), scatter_dimension=1, tiled=True),
        lax.psum_scatter(partials[7], ("fsdp", "ctx"), scatter_dimension=0, tiled=True),
        lax.psum_scatter(partials[8], ("fsdp", "ctx"), scatter_dimension=0, tiled=True),
        lax.psum_scatter(partials[9], ("fsdp", "ctx"), scatter_dimension=0, tiled=True),
        lax.psum_scatter(partials[10], ("fsdp", "ctx"), scatter_dimension=1, tiled=True),
    )
    summed = (
        lax.all_gather(pieces[0], "ctx", axis=0, tiled=True),
        lax.all_gather(pieces[1], "ctx", axis=0, tiled=True),
        lax.all_gather(pieces[2], "ctx", axis=0, tiled=True),
        lax.all_gather(pieces[3], "ctx", axis=0, tiled=True),
        lax.all_gather(pieces[4], "ctx", axis=0, tiled=True),
        lax.all_gather(pieces[5], "ctx", axis=0, tiled=True),
        lax.all_gather(pieces[6], "ctx", axis=1, tiled=True),
        lax.all_gather(pieces[7], "ctx", axis=0, tiled=True),
        lax.all_gather(pieces[8], "ctx", axis=0, tiled=True),
        lax.all_gather(pieces[9], "ctx", axis=0, tiled=True),
        lax.all_gather(pieces[10], "ctx", axis=1, tiled=True),
    )
    return (
        result.astype(jnp.bfloat16),
        teacher_loss,
        tokens_grad,
        summed[0],
        summed[1],
        summed[2],
        summed[3],
        summed[4],
        summed[5],
        summed[6],
        summed[7],
        summed[8],
        summed[9],
        summed[10],
    )


BF16 = jnp.bfloat16
F32 = jnp.float32
LOG2E = math.log2(math.e)
X_SWAP = [(0, 2), (2, 0), (1, 3), (3, 1)]
CORE_SWAP = [(0, 1), (1, 0), (2, 3), (3, 2)]
Y_SWAP = [(0, 1), (1, 0)]
Z_UP = [(0, 1), (1, 2), (2, 3), (3, 0)]
Z_DOWN = [(0, 3), (1, 0), (2, 1), (3, 2)]
Z_NEAR = [(0, 1), (1, 0), (2, 3), (3, 2)]
Z_FAR = [(0, 2), (2, 0), (1, 3), (3, 1)]
MASKS = (0, 2, 1, 3)
ANY = pl.BlockSpec(memory_space=pl.ANY)
SMEM = pl.BlockSpec(memory_space=pltpu.SMEM)


def fits(mesh):
    return dict(mesh.shape) == {"fsdp": 4, "ctx": 2, "tp": 4}


def dot(left, right, left_dim, right_dim):
    return lax.dot_general(
        left, right, (((left_dim,), (right_dim,)), ((), ())), preferred_element_type=F32
    )


def sigmoid(v):
    return 0.5 * jnp.tanh(0.5 * v) + 0.5


def whole(shape):
    zeros = (0,) * len(shape)
    return pl.BlockSpec(shape, lambda *_: zeros, pipeline_mode=pl.Buffered(1))


def settings(dims, mib):
    return pltpu.CompilerParams(
        dimension_semantics=("arbitrary",) * dims, vmem_limit_bytes=mib << 20
    )


def shape_of(shape, dtype):
    return jax.ShapeDtypeStruct(shape, dtype)


def cost(large, microseconds=None):
    size = 1 << 42 if large else 1 << 10
    if microseconds is not None:
        size = int(microseconds * 1.15e9)
    return pl.CostEstimate(flops=size, bytes_accessed=size >> 12, transcendentals=0)


def pack_kernel(info, o_in, g_in, u_in, d_in, *refs):
    out_ref, ffn_ref, *chunk_refs, others_ref, o_ref, g_ref, u_ref, d_ref, sems = refs
    ctx = info[2]
    pairs = ((o_in, o_ref), (g_in, g_ref), (u_in, u_ref), (d_in, d_ref))
    copies = [pltpu.make_async_copy(a, b, sems.at[i]) for i, (a, b) in enumerate(pairs)]
    for copy in copies:
        copy.start()
    for copy in copies:
        copy.wait()
    out_ref[...] = o_ref[...].astype(F32).T.astype(BF16)
    third = g_ref.shape[1] // 3
    for j in range(3):
        at = pl.multiple_of(jnp.where(ctx == 0, j, 2 - j) * third, third)
        parts = [
            g_ref[:, pl.ds(at, third)],
            u_ref[:, pl.ds(at, third)],
            d_ref[pl.ds(at, third), :].astype(F32).T.astype(BF16),
        ]
        for i, part in enumerate(parts):
            chunk_refs[j][:, i * third : (i + 1) * third] = part
            if j:
                others_ref[:, (3 * j - 3 + i) * third : (3 * j - 2 + i) * third] = part
            ffn_ref[:, (3 * j + i) * third : (3 * j + i + 1) * third] = part


def pack(info, o, g, u, d):
    rows, units = g.shape
    feats = o.shape[0]
    widths = (feats, 3 * units, units, units, units, 2 * units)
    return pl.pallas_call(
        pack_kernel,
        in_specs=[SMEM] + [ANY] * 4,
        out_specs=[pl.BlockSpec(memory_space=pltpu.VMEM)] * 6,
        out_shape=[shape_of((rows, n), BF16) for n in widths],
        scratch_shapes=[pltpu.VMEM(a.shape, BF16) for a in (o, g, u, d)]
        + [pltpu.SemaphoreType.DMA((4,))],
        compiler_params=pltpu.CompilerParams(vmem_limit_bytes=24 << 20),
        cost_estimate=cost(False),
        name="pack",
    )(info, o, g, u, d)


def join_kernel(q_ref, k_ref, v_ref, out_ref):
    at = 0
    for ref in (q_ref, k_ref, v_ref):
        out_ref[:, at : at + ref.shape[1]] = ref[...]
        at += ref.shape[1]


def join(q, k, v):
    return pl.pallas_call(
        join_kernel,
        out_shape=shape_of((q.shape[0], q.shape[1] + k.shape[1] + v.shape[1]), BF16),
        compiler_params=pltpu.CompilerParams(vmem_limit_bytes=8 << 20),
        cost_estimate=cost(False),
        name="join",
    )(q, k, v)


def norm_one_kernel(info, tok_ref, gain_ref, x_ref, nt_ref, x32):
    quarter = x_ref.shape[1] // 4
    for p, mask in enumerate(MASKS):
        at = pl.multiple_of(jnp.bitwise_xor(info[1], mask) * quarter, quarter)
        part = tok_ref[0, :, pl.ds(at, quarter)]
        x_ref[:, p * quarter : (p + 1) * quarter] = part
        x32[:, p * quarter : (p + 1) * quarter] = part.astype(F32)
    x = x32[...]
    rho = lax.rsqrt(jnp.mean(x * x, axis=-1, keepdims=True) + EPS)
    nt_ref[...] = (x * rho * gain_ref[...]).T.astype(BF16)


def norm_one(info, tokens, gain, tile):
    _, tok, width = tokens.shape
    return pl.pallas_call(
        norm_one_kernel,
        grid_spec=pltpu.PrefetchScalarGridSpec(
            num_scalar_prefetch=1,
            grid=(tok // tile,),
            in_specs=[
                pl.BlockSpec((1, tile, width), lambda i, info: (info[0], i, 0)),
                pl.BlockSpec((1, width), lambda i, info: (0, 0)),
            ],
            out_specs=[
                pl.BlockSpec((tile, width), lambda i, info: (i, 0)),
                pl.BlockSpec((width, tile), lambda i, info: (0, i)),
            ],
            scratch_shapes=[pltpu.VMEM((tile, width), F32)],
        ),
        out_shape=[shape_of((tok, width), BF16), shape_of((width, tok), BF16)],
        compiler_params=settings(1, 24),
        cost_estimate=cost(False),
        name="norm_one",
    )(info, tokens, gain)


def proj_kernel(heads, block, plan, count, info, *refs):
    nt_ref, cos_ref, sin_ref, qg_ref, kg_ref, rot_ref, raw_ref, w_ref, sem = refs[count:]
    rows = w_ref.shape[0] // 4

    @pl.when(pl.program_id(0) == 0)
    def _():
        for k in range(4):

            @pl.when(block(info) == k)
            def _():
                for p, (piece, row) in enumerate(plan[k]):
                    src = refs[piece].at[pl.ds(row, rows)]
                    pltpu.make_async_copy(src, w_ref.at[pl.ds(p * rows, rows)], sem).start()

        pltpu.make_async_copy(w_ref, w_ref, sem).wait()

    hd = qg_ref.shape[0]
    half = hd // 2
    raw = dot(w_ref[...], nt_ref[...], 0, 0)
    cos_part, sin_part = cos_ref[...], sin_ref[...]
    heads_q, heads_k = heads
    raw_ref[...] = raw.astype(BF16)
    for h in range(heads_q + heads_k):
        v = raw[h * hd : (h + 1) * hd]
        rho = lax.rsqrt(jnp.mean(v * v, axis=0, keepdims=True) + EPS)
        v = v * rho * (qg_ref[...] if h < heads_q else kg_ref[...])
        a, b = v[:half], v[half:]
        rot_ref[h * hd : h * hd + half, :] = (a * cos_part - b * sin_part).astype(BF16)
        rot_ref[h * hd + half : (h + 1) * hd, :] = (b * cos_part + a * sin_part).astype(BF16)
    at = (heads_q + heads_k) * hd
    rot_ref[at:, :] = raw[at:].astype(BF16)


def project(info, weights, normed_t, cos_part, sin_part, gain_q, gain_k, heads, block):
    plan, pieces = weights
    width, tok = normed_t.shape
    cols = pieces[0].shape[1]
    tile = min(512, tok)
    const = lambda a: pl.BlockSpec(a.shape, lambda i, info: (0, 0))
    tab = lambda a: pl.BlockSpec((a.shape[0], tile), lambda i, info: (0, i))
    return pl.pallas_call(
        functools.partial(proj_kernel, heads, block, plan, len(pieces)),
        grid_spec=pltpu.PrefetchScalarGridSpec(
            num_scalar_prefetch=1,
            grid=(tok // tile,),
            in_specs=[ANY] * len(pieces)
            + [tab(normed_t), tab(cos_part), tab(sin_part), const(gain_q), const(gain_k)],
            out_specs=[pl.BlockSpec((cols, tile), lambda i, info: (0, i))] * 2,
            scratch_shapes=[pltpu.VMEM((width, cols), BF16), pltpu.SemaphoreType.DMA],
        ),
        out_shape=[shape_of((cols, tok), BF16), shape_of((cols, tok), BF16)],
        compiler_params=settings(1, 24),
        cost_estimate=cost(False),
        name="project",
    )(info, *pieces, normed_t, cos_part, sin_part, gain_q, gain_k)


def head_back_kernel(
    heads, info, dm_ref, dt_ref, rm_ref, rt_ref, cos_ref, sin_ref, qg_ref, kg_ref, out_ref, gg_ref
):
    step, part = pl.program_id(0), pl.program_id(1)
    hd = qg_ref.shape[0]
    half = hd // 2
    heads_q, heads_k = heads
    cos_part, sin_part = cos_ref[...], sin_ref[...]
    tile = cos_part.shape[1]

    @pl.when((step == 0) & (part == 0))
    def _():
        gg_ref[...] = jnp.zeros_like(gg_ref)

    def work(d_ref, r_ref):
        gain_q = jnp.zeros((hd, 1), F32)
        gain_k = jnp.zeros((hd, 1), F32)
        done = []
        for h in range(heads_q + heads_k):
            is_q = h < heads_q
            g = d_ref[h * hd : (h + 1) * hd, :].astype(F32)
            raw = r_ref[h * hd : (h + 1) * hd, :].astype(F32)
            a, b = g[:half], g[half:]
            turned = jnp.concatenate(
                [a * cos_part + b * sin_part, b * cos_part - a * sin_part], axis=0
            )
            rho = lax.rsqrt(jnp.mean(raw * raw, axis=0, keepdims=True) + EPS)
            unit = raw * rho
            prod = turned * unit
            scaled = turned * (qg_ref[...] if is_q else kg_ref[...])
            mean = jnp.mean(scaled * unit, axis=0, keepdims=True)
            done.append(rho * (scaled - unit * mean))
            total = jnp.sum(prod, axis=1, keepdims=True)
            if is_q:
                gain_q = gain_q + total
            else:
                gain_k = gain_k + total
        done.append(d_ref[(heads_q + heads_k) * hd :, :].astype(F32))
        out_ref[0] = jnp.concatenate(done, axis=0).T.astype(BF16)
        lane = lax.broadcasted_iota(jnp.int32, gg_ref.shape, 1)
        gg_ref[...] += jnp.where(lane == 0, gain_q, jnp.where(lane == 1, gain_k, 0.0))

    @pl.when(step == 0)
    def _():
        work(dm_ref, rm_ref)

    @pl.when(step == 1)
    def _():
        work(dt_ref, rt_ref)


def head_back(info, grad_mine, grad_theirs, raw_mine, raw_theirs, cos_part, sin_part, gq, gk, heads):
    cols, tok = grad_mine.shape
    tile = min(512, tok)
    mine = pl.BlockSpec((cols, tile), lambda s, i, info: (0, jnp.where(s == 0, i, tok // tile - 1)))
    theirs = pl.BlockSpec((cols, tile), lambda s, i, info: (0, jnp.where(s == 0, 0, i)))
    tab = lambda a: pl.BlockSpec((a.shape[0], tile), lambda s, i, info: (0, i))
    const = lambda a: pl.BlockSpec(a.shape, lambda s, i, info: (0, 0))
    return pl.pallas_call(
        functools.partial(head_back_kernel, heads),
        grid_spec=pltpu.PrefetchScalarGridSpec(
            num_scalar_prefetch=1,
            grid=(2, tok // tile),
            in_specs=[
                mine,
                theirs,
                mine,
                theirs,
                tab(cos_part),
                tab(sin_part),
                const(gq),
                const(gk),
            ],
            out_specs=[
                pl.BlockSpec(
                    (1, tile, cols), lambda s, i, info: (jnp.bitwise_xor(info[2], s), i, 0)
                ),
                pl.BlockSpec((gq.shape[0], 128), lambda s, i, info: (0, 0)),
            ],
        ),
        out_shape=[shape_of((2, tok, cols), BF16), shape_of((gq.shape[0], 128), F32)],
        compiler_params=settings(2, 60),
        cost_estimate=cost(False),
        name="head_back",
    )(info, grad_mine, grad_theirs, raw_mine, raw_theirs, cos_part, sin_part, gq, gk)


def load_rows(info, mine_ref, got_ref, rows, sems):
    tok = mine_ref.shape[1]
    ctx = info[2]
    here = pl.multiple_of(ctx * tok, tok)
    there = pl.multiple_of((1 - ctx) * tok, tok)
    one = pltpu.make_async_copy(mine_ref, rows.at[:, pl.ds(here, tok)], sems.at[0])
    two = pltpu.make_async_copy(got_ref, rows.at[:, pl.ds(there, tok)], sems.at[1])
    one.start()
    two.start()
    one.wait()
    two.wait()


def keys_with_bias(keys, length):
    hd, slots = keys.shape
    pos = lax.broadcasted_iota(jnp.int32, (hd, slots), 1)
    row = lax.broadcasted_iota(jnp.int32, (hd, slots), 0)
    bias = jnp.where((row == 0) & (pos >= length), NEGATIVE, 0.0)
    return jnp.concatenate([keys.astype(F32), bias], axis=0).T.astype(BF16)


def query_with_one(pair):
    one_row = jnp.where(lax.broadcasted_iota(jnp.int32, pair.shape, 0) == 0, 1.0, 0.0)
    return jnp.concatenate([pair, one_row.astype(BF16)], axis=0)


def by_halves(left, right):
    half = left.shape[1] // 2
    return jnp.concatenate(
        [left[:, :half], right[:, :half], left[:, half:], right[:, half:]], axis=1
    )


def by_heads(both):
    quarter = both.shape[1] // 4
    part = lambda i: both[:, i * quarter : (i + 1) * quarter]
    return (
        jnp.concatenate([part(0), part(2)], axis=1),
        jnp.concatenate([part(1), part(3)], axis=1),
    )


def causal(scores):
    half = scores.shape[0]
    key_pos = lax.broadcasted_iota(jnp.int32, (half, half), 0)
    query_pos = lax.broadcasted_iota(jnp.int32, (half, half), 1)
    allowed = key_pos <= query_pos
    return jnp.where(jnp.concatenate([allowed, allowed], axis=1), scores, NEGATIVE)


def attn_fwd_kernel(
    width, hd, info, mine_ref, got_ref, keep_ref, send_ref, lse_ref, rows, key_rows, sems
):
    head, block = pl.program_id(0), pl.program_id(1)
    heads_k = pl.num_programs(0)
    scale = hd**-0.5 * LOG2E
    length = info[3]
    key_at = pl.multiple_of(heads_k * 2 * hd + head * hd, hd)
    value_at = pl.multiple_of(heads_k * 3 * hd + head * hd, hd)
    query_at = pl.multiple_of(head * 2 * hd, 2 * hd)

    @pl.when((head == 0) & (block == 0))
    def _():
        load_rows(info, mine_ref, got_ref, rows, sems)

    @pl.when(block == 0)
    def _():
        key_rows[...] = keys_with_bias(rows[pl.ds(key_at, hd), :], length)

    start = pl.multiple_of(block * width, width)
    both = rows[pl.ds(query_at, 2 * hd), pl.ds(start, width)]
    query = query_with_one(by_halves(both[:hd], both[hd:]))

    def tile(at, carried, diagonal):
        out, total = carried
        scores = dot(key_rows[pl.ds(at, width), :], query, 1, 0)
        if diagonal:
            key_pos = lax.broadcasted_iota(jnp.int32, (width, width), 0)
            query_pos = lax.broadcasted_iota(jnp.int32, (width, width), 1)
            allowed = key_pos <= query_pos
            allowed = by_halves(allowed, allowed)
            scores = jnp.where(allowed, scores, NEGATIVE)
        probs = jnp.exp2(scores * scale)
        total = total + jnp.sum(probs, axis=0, keepdims=True)
        out = out + dot(rows[pl.ds(value_at, hd), pl.ds(at, width)], probs.astype(BF16), 1, 0)
        return out, total

    carried = (jnp.zeros((hd, 2 * width), F32), jnp.zeros((1, 2 * width), F32))
    full = jnp.minimum(block, lax.div(length + width - 1, width))
    carried = lax.fori_loop(
        0, full, lambda j, c: tile(pl.multiple_of(j * width, width), c, False), carried
    )
    out, total = tile(start, carried, True)
    out = out * (1.0 / total)
    out = jnp.concatenate(by_heads(out), axis=0).T.astype(BF16)
    here = block // 2 == info[2]

    @pl.when(here)
    def _():
        keep_ref[...] = out

    @pl.when(jnp.logical_not(here))
    def _():
        send_ref[...] = out

    log_first, log_second = by_heads(jnp.log2(total))
    lse_ref[0, 0:1, :] = log_first
    lse_ref[0, 1:2, :] = log_second


def keep_block(i, info):
    return jnp.clip(i - 2 * info[2], 0, 1)


def send_block(i, info):
    return jnp.clip(i - 2 * (1 - info[2]), 0, 1)


def attn_fwd(info, mine, got, hd):
    cols, tok = mine.shape
    heads_k = cols // (4 * hd)
    width = tok // 2
    return pl.pallas_call(
        functools.partial(attn_fwd_kernel, width, hd),
        grid_spec=pltpu.PrefetchScalarGridSpec(
            num_scalar_prefetch=1,
            grid=(heads_k, 4),
            in_specs=[ANY, ANY],
            out_specs=[
                pl.BlockSpec((width, 2 * hd), lambda h, i, info: (keep_block(i, info), h)),
                pl.BlockSpec((width, 2 * hd), lambda h, i, info: (send_block(i, info), h)),
                pl.BlockSpec((1, 2, width), lambda h, i, info: (h, 0, i)),
            ],
            scratch_shapes=[
                pltpu.VMEM((cols, 2 * tok), BF16),
                pltpu.VMEM((2 * tok, 2 * hd), BF16),
                pltpu.SemaphoreType.DMA((2,)),
            ],
        ),
        out_shape=[
            shape_of((tok, heads_k * 2 * hd), BF16),
            shape_of((tok, heads_k * 2 * hd), BF16),
            shape_of((heads_k, 2, 2 * tok), F32),
        ],
        compiler_params=settings(2, 60),
        cost_estimate=cost(True),
        name="attn_fwd",
    )(info, mine, got)


def attn_bwd_kernel(
    width,
    hd,
    info,
    mine_ref,
    got_ref,
    ok_ref,
    os_ref,
    gk_ref,
    gs_ref,
    lse_ref,
    keep_ref,
    send_ref,
    rows,
    key_rows,
    value_rows,
    key_sum,
    value_sum,
    sems,
):
    head, block = pl.program_id(0), pl.program_id(1)
    heads_k = pl.num_programs(0)
    scale = hd**-0.5
    length = info[3]
    ctx = info[2]
    tok = keep_ref.shape[1]
    key_at = pl.multiple_of(heads_k * 2 * hd + head * hd, hd)
    value_at = pl.multiple_of(heads_k * 3 * hd + head * hd, hd)
    query_at = pl.multiple_of(head * 2 * hd, 2 * hd)

    @pl.when((head == 0) & (block == 0))
    def _():
        load_rows(info, mine_ref, got_ref, rows, sems)

    @pl.when(block == 0)
    def _():
        key_rows[...] = keys_with_bias(rows[pl.ds(key_at, hd), :], length)
        value_rows[...] = rows[pl.ds(value_at, hd), :].astype(F32).T.astype(BF16)
        key_sum[...] = jnp.zeros_like(key_sum)
        value_sum[...] = jnp.zeros_like(value_sum)

    start = pl.multiple_of(block * width, width)
    here = block // 2 == ctx

    def store_query(value):
        at = pl.ds(pl.multiple_of((block % 2) * width, width), width)

        @pl.when(here)
        def _():
            keep_ref[pl.ds(query_at, 2 * hd), at] = value

        @pl.when(jnp.logical_not(here))
        def _():
            send_ref[pl.ds(query_at, 2 * hd), at] = value

    @pl.when(block * width < length)
    def _():
        both = rows[pl.ds(query_at, 2 * hd), pl.ds(start, width)]
        pair = by_halves(both[:hd], both[hd:])
        query = query_with_one(pair)
        query_rows = pair.astype(F32).T.astype(BF16)
        grad_wide = jnp.where(here, gk_ref[...].astype(F32), gs_ref[...].astype(F32))
        out_wide = jnp.where(here, ok_ref[...].astype(F32), os_ref[...].astype(F32))
        grad_t = grad_wide.T
        prod = (grad_wide * out_wide).T
        grad = by_halves(grad_t[:hd], grad_t[hd:]).astype(BF16)
        half = width // 2
        grad_rows = jnp.concatenate(
            [
                grad_wide[:half, :hd],
                grad_wide[:half, hd:],
                grad_wide[half:, :hd],
                grad_wide[half:, hd:],
            ],
            axis=0,
        ).astype(BF16)
        delta = by_halves(
            jnp.sum(prod[:hd], axis=0, keepdims=True), jnp.sum(prod[hd:], axis=0, keepdims=True)
        )
        lse = by_halves(lse_ref[0, 0:1, :], lse_ref[0, 1:2, :])

        def terms(at, keys, first, mask):
            scores = dot(key_rows[pl.ds(at, keys), :], query[:, first:], 1, 0)
            if mask:
                part = causal(scores[:, :width])
                wide = scores.shape[1] > width
                scores = jnp.concatenate([part, scores[:, width:]], axis=1) if wide else part
            probs = jnp.exp2(scores * (scale * LOG2E) - lse[:, first:])
            grad_probs = dot(value_rows[pl.ds(at, keys), :], grad[:, first:], 1, 0)
            grad_scores = (probs * (grad_probs - delta[:, first:])).astype(BF16)
            value_sum[pl.ds(at, keys), :] += dot(probs.astype(BF16), grad_rows[first:], 1, 0)
            key_sum[pl.ds(at, keys), :] += dot(grad_scores, query_rows[first:], 1, 0)
            return dot(rows[pl.ds(key_at, hd), pl.ds(at, keys)], grad_scores, 1, 0)

        query_sum = lax.fori_loop(
            0,
            block,
            lambda j, s: s + terms(pl.multiple_of(j * width, width), width, 0, False),
            jnp.zeros((hd, 2 * width), F32),
        )
        query_sum = query_sum + terms(start, half, 0, True)
        later = terms(pl.multiple_of(start + half, half), half, width, True)
        query_sum = jnp.concatenate([query_sum[:, :width], query_sum[:, width:] + later], axis=1)
        store_query(jnp.concatenate(by_heads(query_sum * scale), axis=0).astype(BF16))

    @pl.when(block * width >= length)
    def _():
        store_query(jnp.zeros((2 * hd, width), BF16))

    @pl.when(block == 3)
    def _():
        for at, total in ((key_at, key_sum[...] * scale), (value_at, value_sum[...])):
            total = total.T.astype(BF16)
            left, right = total[:, :tok], total[:, tok:]

            @pl.when(ctx == 0)
            def _():
                keep_ref[pl.ds(at, hd), :] = left
                send_ref[pl.ds(at, hd), :] = right

            @pl.when(ctx == 1)
            def _():
                keep_ref[pl.ds(at, hd), :] = right
                send_ref[pl.ds(at, hd), :] = left


def attn_bwd(info, mine, got, out_keep, out_send, grad_keep, grad_send, lse, hd):
    cols, tok = mine.shape
    heads_k = cols // (4 * hd)
    width = tok // 2
    keep = pl.BlockSpec((width, 2 * hd), lambda h, i, info: (keep_block(i, info), h))
    send = pl.BlockSpec((width, 2 * hd), lambda h, i, info: (send_block(i, info), h))
    full = pl.BlockSpec((cols, tok), lambda h, i, info: (0, 0))
    return pl.pallas_call(
        functools.partial(attn_bwd_kernel, width, hd),
        grid_spec=pltpu.PrefetchScalarGridSpec(
            num_scalar_prefetch=1,
            grid=(heads_k, 4),
            in_specs=[
                ANY,
                ANY,
                keep,
                send,
                keep,
                send,
                pl.BlockSpec((1, 2, width), lambda h, i, info: (h, 0, i)),
            ],
            out_specs=[full, full],
            scratch_shapes=[
                pltpu.VMEM((cols, 2 * tok), BF16),
                pltpu.VMEM((2 * tok, 2 * hd), BF16),
                pltpu.VMEM((2 * tok, hd), BF16),
                pltpu.VMEM((2 * tok, hd), F32),
                pltpu.VMEM((2 * tok, hd), F32),
                pltpu.SemaphoreType.DMA((2,)),
            ],
        ),
        out_shape=[shape_of((cols, tok), BF16), shape_of((cols, tok), BF16)],
        compiler_params=settings(2, 60),
        cost_estimate=cost(True, 16.2),
        name="attn_bwd",
    )(info, mine, got, out_keep, out_send, grad_keep, grad_send, lse)


def load_blocks(plan, pieces, target, sem):
    rows = target.shape[1] // 4

    @pl.when(pl.program_id(0) == 0)
    def _():
        for k, places in enumerate(plan):
            for p, (piece, row) in enumerate(places):
                src = pieces[piece].at[pl.ds(row, rows)]
                pltpu.make_async_copy(src, target.at[k, pl.ds(p * rows, rows)], sem).start()
        pltpu.make_async_copy(target, target, sem).wait()


def out_proj_kernel(plan, count, info, *refs):
    x_ref, a0, a1, b0, b1, gain_ref, r_ref, n_ref, nt_ref, att_ref, w_ref, sem = refs[count:]
    load_blocks(plan, refs, w_ref, sem)
    ctx = info[2]
    total = x_ref[...].astype(F32)
    for j, ref, side in ((0, a0, ctx), (1, a1, ctx), (0, b0, 1 - ctx), (1, b1, 1 - ctx)):
        block = 2 * side + j
        part = ref[...]
        att_ref[block] = part
        total = total + dot(part, w_ref[block], 1, 1)
    rho = lax.rsqrt(jnp.mean(total * total, axis=-1, keepdims=True) + EPS)
    normed = total * rho * gain_ref[...]
    r_ref[...] = total
    n_ref[...] = normed.astype(BF16)
    nt_ref[...] = normed.T.astype(BF16)


def out_proj(info, x, mine, theirs, weights, gain, tile):
    plan, pieces = weights
    tok, width = x.shape
    feats = pieces[0].shape[1]
    rows_of = lambda n: pl.BlockSpec((tile, n), lambda i, info: (i, 0))
    return pl.pallas_call(
        functools.partial(out_proj_kernel, plan, len(pieces)),
        grid_spec=pltpu.PrefetchScalarGridSpec(
            num_scalar_prefetch=1,
            grid=(tok // tile,),
            in_specs=[ANY] * len(pieces)
            + [rows_of(width)]
            + [rows_of(feats)] * 4
            + [pl.BlockSpec((1, width), lambda i, info: (0, 0))],
            out_specs=[
                rows_of(width),
                rows_of(width),
                pl.BlockSpec((width, tile), lambda i, info: (0, i)),
                pl.BlockSpec((4, tile, feats), lambda i, info: (0, i, 0)),
            ],
            scratch_shapes=[pltpu.VMEM((4, width, feats), BF16), pltpu.SemaphoreType.DMA],
        ),
        out_shape=[
            shape_of((tok, width), F32),
            shape_of((tok, width), BF16),
            shape_of((width, tok), BF16),
            shape_of((4, tok, feats), BF16),
        ],
        compiler_params=settings(1, 60),
        cost_estimate=cost(True),
        name="out_proj",
    )(info, *pieces, x, *mine, *theirs, gain)


def norm_two_back_kernel(plan, count, info, *refs):
    g_ref, r_ref, gr_ref, gain_ref, gres_ref, gat_ref, a0, a1, b0, b1, gg_ref, w_ref, sem = refs[count:]
    load_blocks(plan, refs, w_ref, sem)
    ctx = info[2]
    grad, resid = g_ref[...], r_ref[...]
    rho = lax.rsqrt(jnp.mean(resid * resid, axis=-1, keepdims=True) + EPS)
    unit = resid * rho
    scaled = grad * gain_ref[...]
    back = rho * (scaled - unit * jnp.mean(scaled * unit, axis=-1, keepdims=True))
    total = gr_ref[...].astype(F32) + back
    low = total.astype(BF16)
    gres_ref[...] = low
    gat_ref[...] = total.T.astype(BF16)

    @pl.when(pl.program_id(0) == 0)
    def _():
        gg_ref[...] = jnp.zeros_like(gg_ref)

    gg_ref[...] += jnp.sum(grad * unit, axis=0, keepdims=True)
    for j, ref, side in ((0, a0, ctx), (1, a1, ctx), (0, b0, 1 - ctx), (1, b1, 1 - ctx)):
        ref[...] = dot(low, w_ref[2 * side + j], 1, 0).astype(BF16)


def norm_two_back(info, grad, resid, grad_result, gain, weights, tile):
    plan, pieces = weights
    tok, width = grad.shape
    feats = pieces[0].shape[1]
    rows_of = lambda n: pl.BlockSpec((tile, n), lambda i, info: (i, 0))
    row = pl.BlockSpec((1, width), lambda i, info: (0, 0))
    return pl.pallas_call(
        functools.partial(norm_two_back_kernel, plan, len(pieces)),
        grid_spec=pltpu.PrefetchScalarGridSpec(
            num_scalar_prefetch=1,
            grid=(tok // tile,),
            in_specs=[ANY] * len(pieces) + [rows_of(width)] * 3 + [row],
            out_specs=[rows_of(width), pl.BlockSpec((width, tile), lambda i, info: (0, i))]
            + [rows_of(feats)] * 4
            + [row],
            scratch_shapes=[pltpu.VMEM((4, width, feats), BF16), pltpu.SemaphoreType.DMA],
        ),
        out_shape=[shape_of((tok, width), BF16), shape_of((width, tok), BF16)]
        + [shape_of((tok, feats), BF16)] * 4
        + [shape_of((1, width), F32)],
        compiler_params=settings(1, 60),
        cost_estimate=cost(True, 5.4),
        name="norm_two_back",
    )(info, *pieces, grad, resid, grad_result, gain)


def norm_one_back_kernel(plan, count, info, *refs):
    p0, p1, x_ref, gres_ref, gain_ref, out_ref, gg_ref, w_ref, sem = refs[count:]
    load_blocks(plan, refs, w_ref, sem)
    quarter = x_ref.shape[1] // 4
    grad = dot(p0[0], w_ref[0], 1, 1)
    grad = grad + dot(p1[0], w_ref[1], 1, 1)
    grad = grad + dot(p0[1], w_ref[2], 1, 1)
    grad = grad + dot(p1[1], w_ref[3], 1, 1)
    x = x_ref[...].astype(F32)
    rho = lax.rsqrt(jnp.mean(x * x, axis=-1, keepdims=True) + EPS)
    unit = x * rho
    scaled = grad * gain_ref[...]
    back = rho * (scaled - unit * jnp.mean(scaled * unit, axis=-1, keepdims=True))
    total = (gres_ref[...].astype(F32) + back).astype(BF16)
    for p, mask in enumerate(MASKS):
        at = pl.multiple_of(jnp.bitwise_xor(info[1], mask) * quarter, quarter)
        part = total[:, p * quarter : (p + 1) * quarter]

        out_ref[:, pl.ds(at, quarter)] = part

    @pl.when(pl.program_id(0) == 0)
    def _():
        gg_ref[...] = jnp.zeros_like(gg_ref)

    gg_ref[...] += jnp.sum(grad * unit, axis=0, keepdims=True)


def norm_one_back(info, pairs, weights, x, grad_resid, gain, tile, part):
    plan, pieces = weights
    tok, width = x.shape
    cols = pieces[0].shape[1]
    steps = tok // tile // 2
    first = part * steps
    rows_of = lambda n: pl.BlockSpec((tile, n), lambda i, info: (first + i, 0))
    out_rows = pl.BlockSpec((tile, width), lambda i, info: (i, 0))
    pair = pl.BlockSpec((2, tile, cols), lambda i, info: (0, first + i, 0))
    row = pl.BlockSpec((1, width), lambda i, info: (0, 0))
    return pl.pallas_call(
        functools.partial(norm_one_back_kernel, plan, len(pieces)),
        grid_spec=pltpu.PrefetchScalarGridSpec(
            num_scalar_prefetch=1,
            grid=(steps,),
            in_specs=[ANY] * len(pieces) + [pair, pair, rows_of(width), rows_of(width), row],
            out_specs=[out_rows, row],
            scratch_shapes=[pltpu.VMEM((4, width, cols), BF16), pltpu.SemaphoreType.DMA],
        ),
        out_shape=[shape_of((tok // 2, width), BF16), shape_of((1, width), F32)],
        compiler_params=settings(1, 60),
        cost_estimate=cost(True),
        name="norm_one_back",
    )(info, *pieces, *pairs, x, grad_resid, gain)


def weight_copies(plan, pieces, gate_up, down, gate_up_sem, down_sem):
    third = down.shape[1] // 3
    rows = down.shape[0] // 4
    wide, thin = [], []
    for p, chunks in enumerate(plan):
        block = pl.ds(p * rows, rows)
        for j, (piece, row, at) in enumerate(chunks):
            src = pieces[piece].at[pl.ds(row, rows)]
            wide.append(
                pltpu.make_async_copy(
                    src.at[:, pl.ds(at, 2 * third)],
                    gate_up.at[block, pl.ds(j * 2 * third, 2 * third)],
                    gate_up_sem,
                )
            )
            thin.append(
                pltpu.make_async_copy(
                    src.at[:, pl.ds(at + 2 * third, third)],
                    down.at[block, pl.ds(j * third, third)],
                    down_sem,
                )
            )
    return wide, thin


def split_act(act):
    third = act.shape[1] // 6
    part = lambda j: act[:, j * third : (j + 1) * third]
    return [(part(0), part(1)), (part(2), part(3)), (part(4), part(5))]


def ffn_fwd_kernel(tile, plans, last, info, scale, x_ref, in_ref, *rest):
    if last:
        teach_ref, rest = rest[0], rest[1:]
    pieces = []
    for plan in plans:
        count = 1 + max(place[0] for chunks in plan for place in chunks)
        pieces.append(rest[:count])
        rest = rest[count:]
    act_ref, hid_ref = rest[:2]
    if last:
        out_ref, low_ref, lowt_ref, sq_ref = rest[2:6]
        gate_up, down, total, sems = rest[6:]
    else:
        sum_ref, gate_up, down, total, sems = rest[2:]
    step, part = pl.program_id(0), pl.program_id(1)
    final = len(plans) - 1
    width = x_ref.shape[1]
    quarter = width // 4
    third = down.shape[2] // 3

    def copies(s):
        return weight_copies(
            plans[s], pieces[s], gate_up.at[s], down.at[s], sems.at[s, 0], sems.at[s, 1]
        )

    @pl.when((step == 0) & (part == 0))
    def _():
        for s in range(len(plans)):
            wide, thin = copies(s)
            for copy in wide + thin:
                copy.start()

    for s in range(len(plans)):

        @pl.when((step == s) & (part == 0))
        def _():
            pltpu.make_async_copy(gate_up.at[s], gate_up.at[s], sems.at[s, 0]).wait()

    rows = pl.ds(pl.multiple_of(part * tile, tile), tile)
    act = dot(x_ref[rows, :], gate_up[step], 1, 0)
    for j, (gate, upper) in enumerate(split_act(act)):
        sig = sigmoid(gate)
        silu = gate * sig
        hid_ref[0, :, j * third : (j + 1) * third] = (silu * upper).astype(BF16)
        at = 2 * j * third
        act_ref[0, :, at : at + third] = (upper * (sig + silu - silu * sig)).astype(BF16)
        act_ref[0, :, at + third : at + 2 * third] = silu.astype(BF16)
    for s in range(len(plans)):

        @pl.when((step == s) & (part == 0))
        def _():
            pltpu.make_async_copy(down.at[s], down.at[s], sems.at[s, 1]).wait()

    grown = dot(hid_ref[0], down[step], 1, 1)

    @pl.when(step == 0)
    def _():
        total[rows, :] = in_ref[...] + grown

    @pl.when(step > 0)
    def _():
        total[rows, :] += grown

    @pl.when(step == final)
    def _():
        result = total[rows, :]
        if not last:
            sum_ref[...] = result
            return
        tok = x_ref.shape[0]
        slot = info[2] * tok + part * tile + lax.broadcasted_iota(jnp.int32, (tile, 1), 0)
        valid = jnp.where(slot < info[3], 1.0, 0.0)
        square = jnp.zeros((tile, quarter), F32)
        for p, mask in enumerate(MASKS):
            at = pl.multiple_of(jnp.bitwise_xor(info[1], mask) * quarter, quarter)
            cols = slice(p * quarter, (p + 1) * quarter)
            value = result[:, cols]
            out_ref[:, pl.ds(at, quarter)] = value.astype(BF16)
            error = valid * (value - teach_ref[0, :, pl.ds(at, quarter)].astype(F32))
            square = square + error * error
            grad = error * scale[0]
            low_ref[:, cols] = grad.astype(BF16)
            lowt_ref[cols, :] = grad.T.astype(BF16)

        @pl.when(part == 0)
        def _():
            sq_ref[...] = jnp.zeros_like(sq_ref)

        sq_ref[...] += jnp.sum(square, axis=0, keepdims=True)


def ffn_fwd(info, scale, x, total, teacher, weights, units, tile):
    tok, width = x.shape
    pieces = [piece for _, group in weights for piece in group]
    count = len(weights)
    last = teacher is not None
    entry = lambda s, i: jnp.where(s == 0, i, tok // tile - 1)
    leave = lambda s, i: jnp.where(s == count - 1, i, 0)
    tiles = lambda n: pl.BlockSpec((tile, n), lambda s, i, info: (leave(s, i), 0))
    slab = lambda n: pl.BlockSpec((1, tile, n), lambda s, i, info: (s, i, 0))
    in_specs = [
        SMEM,
        whole((tok, width)),
        pl.BlockSpec((tile, width), lambda s, i, info: (entry(s, i), 0)),
    ]
    out_specs = [slab(2 * units), slab(units)]
    out_shape = [shape_of((count, tok, 2 * units), BF16), shape_of((count, tok, units), BF16)]
    if last:
        in_specs.append(
            pl.BlockSpec((1, tile, width), lambda s, i, info: (info[0], leave(s, i), 0))
        )
        out_specs += [
            tiles(width),
            tiles(width),
            pl.BlockSpec((width, tile), lambda s, i, info: (0, leave(s, i))),
            pl.BlockSpec((1, width // 4), lambda s, i, info: (0, 0)),
        ]
        out_shape += [
            shape_of((tok, width), BF16),
            shape_of((tok, width), BF16),
            shape_of((width, tok), BF16),
            shape_of((1, width // 4), F32),
        ]
    else:
        out_specs.append(tiles(width))
        out_shape.append(shape_of((tok, width), F32))
    return pl.pallas_call(
        functools.partial(ffn_fwd_kernel, tile, [plan for plan, _ in weights], last),
        grid_spec=pltpu.PrefetchScalarGridSpec(
            num_scalar_prefetch=1,
            grid=(count, tok // tile),
            in_specs=in_specs + [ANY] * len(pieces),
            out_specs=out_specs,
            scratch_shapes=[
                pltpu.VMEM((count, width, 2 * units), BF16),
                pltpu.VMEM((count, width, units), BF16),
                pltpu.VMEM((tok, width), F32),
                pltpu.SemaphoreType.DMA((count, 2)),
            ],
        ),
        out_shape=out_shape,
        compiler_params=settings(2, 60),
        cost_estimate=cost(True),
        name="ffn_fwd",
    )(info, scale, x, total, *([teacher] if last else []), *pieces)


def ffn_bwd_kernel(steps, plan, first, low_ref, act_ref, hid_ref, xt_ref, lowt_ref, *rest):
    count = 1 + max(place[0] for chunks in plan for place in chunks)
    pieces, rest = rest[:count], rest[count:]
    if not first:
        in_ref, rest = rest[0], rest[1:]
    out_ref, keep_ref, send_ref, gate_up, down, dact_all, hid_all, sems = rest
    step = pl.program_id(0)
    units = down.shape[1]
    third = units // 3
    tile = low_ref.shape[0]

    @pl.when(step == 0)
    def _():
        wide, thin = weight_copies(plan, pieces, gate_up, down, sems.at[0], sems.at[1])
        for copy in thin + wide:
            copy.start()
        pltpu.make_async_copy(down, down, sems.at[1]).wait()

    @pl.when(step < steps)
    def _():
        rows = pl.ds(pl.multiple_of(step * tile, tile), tile)
        grad_hidden = dot(low_ref[...], down[...], 1, 0)
        for j, (to_gate, to_upper) in enumerate(split_act(act_ref[0])):
            grad = grad_hidden[:, j * third : (j + 1) * third]
            at = 2 * j * third
            dact_all[rows, at : at + third] = (grad * to_gate.astype(F32)).astype(BF16)
            dact_all[rows, at + third : at + 2 * third] = (grad * to_upper.astype(F32)).astype(BF16)
        hid_all[rows, :] = hid_ref[0]

        @pl.when(step == 0)
        def _():
            pltpu.make_async_copy(gate_up, gate_up, sems.at[0]).wait()

        grown = dot(dact_all[rows, :], gate_up[...], 1, 1)
        out_ref[...] = grown if first else in_ref[...] + grown

    def weight_rows(target):
        target[:, : 2 * units] = dot(xt_ref[...], dact_all[...], 1, 0).astype(BF16)
        target[:, 2 * units :] = dot(lowt_ref[...], hid_all[...], 1, 0).astype(BF16)

    @pl.when((step >= steps) & (step < steps + 2))
    def _():
        weight_rows(send_ref)

    @pl.when(step >= steps + 2)
    def _():
        weight_rows(keep_ref)


def ffn_bwd(low, saved, weights, total, xt, lowt, tile):
    plan, pieces = weights
    acts, hiddens, block = saved
    tok, width = low.shape
    units = hiddens.shape[2]
    steps = tok // tile
    quarter = width // 4
    first = total is None
    clip = lambda i: jnp.minimum(i, steps - 1)
    rows_of = lambda n: pl.BlockSpec((tile, n), lambda i: (clip(i), 0))
    slab = lambda n: pl.BlockSpec((1, tile, n), lambda i: (block, clip(i), 0))
    feature = lambda i: (jnp.where(i < steps + 2, jnp.maximum(i - steps, 0) + 2, i - steps - 2), 0)
    return pl.pallas_call(
        functools.partial(ffn_bwd_kernel, steps, plan, first),
        grid=(steps + 4,),
        in_specs=[
            rows_of(width),
            slab(2 * units),
            slab(units),
            pl.BlockSpec((quarter, tok), feature),
            pl.BlockSpec((quarter, tok), feature),
        ]
        + [ANY] * len(pieces)
        + ([] if first else [rows_of(width)]),
        out_specs=[
            rows_of(width),
            pl.BlockSpec((quarter, 3 * units), lambda i: (jnp.maximum(i - steps - 2, 0), 0)),
            pl.BlockSpec((quarter, 3 * units), lambda i: (jnp.clip(i - steps, 0, 1), 0)),
        ],
        out_shape=[
            shape_of((tok, width), F32),
            shape_of((width // 2, 3 * units), BF16),
            shape_of((width // 2, 3 * units), BF16),
        ],
        scratch_shapes=[
            pltpu.VMEM((width, 2 * units), BF16),
            pltpu.VMEM((width, units), BF16),
            pltpu.VMEM((tok, 2 * units), BF16),
            pltpu.VMEM((tok, units), BF16),
            pltpu.SemaphoreType.DMA((2,)),
        ],
        input_output_aliases={} if first else {5 + len(pieces): 0},
        compiler_params=settings(1, 60),
        cost_estimate=cost(True, 11.2),
        name="ffn_bwd",
    )(low, acts, hiddens, xt, lowt, *pieces, *([] if first else [total]))


def turn_chunks(block):
    wide = block.shape[1] * 2 // 9
    thin = wide // 2
    starts = [(2 * wide, wide), (wide, wide), (0, wide)]
    starts += [(3 * wide + 2 * thin, thin), (3 * wide + thin, thin), (3 * wide, thin)]
    return jnp.concatenate([block[:, a : a + n] for a, n in starts], axis=1)


def sum_kernel(turns, *refs):
    total = None
    for ref, turn in zip(refs[:-1], turns):
        value = ref[...].astype(F32)
        value = turn_chunks(value) if turn else value
        total = value if total is None else total + value
    refs[-1][...] = total.astype(refs[-1].dtype)


def summed(terms, turns=None, dtype=BF16):
    rows, cols = terms[0].shape
    spec = pl.BlockSpec((128, cols), lambda i: (i, 0))
    return pl.pallas_call(
        functools.partial(sum_kernel, turns or [False] * len(terms)),
        grid=(rows // 128,),
        in_specs=[spec] * len(terms),
        out_specs=spec,
        out_shape=shape_of((rows, cols), dtype),
        compiler_params=settings(1, 60),
        cost_estimate=cost(False),
        name="summed",
    )(*terms)


def sums_kernel(jobs, count, info, *refs):
    arrays, refs = refs[:count], refs[count:]
    outs, (term_buf, out_buf, term_sems, out_sems) = refs[: len(jobs)], refs[len(jobs) :]
    rows = term_buf.shape[1]
    copies = []
    for terms in jobs:
        group = []
        for array, base, pick, _ in terms:
            at = base
            if pick is not None:
                at = pl.multiple_of(base + jnp.bitwise_xor(info[2], pick) * rows, rows)
            i = len(copies) + len(group)
            src = arrays[array].at[pl.ds(at, rows)]
            group.append(pltpu.make_async_copy(src, term_buf.at[i], term_sems.at[i]))
            group[-1].start()
        copies += group
    first = 0
    stores = []
    for j, terms in enumerate(jobs):
        total = None
        for i, (_, _, _, turn) in enumerate(terms):
            copies[first + i].wait()
            value = term_buf[first + i].astype(F32)
            value = turn_chunks(value) if turn else value
            total = value if total is None else total + value
        first += len(terms)
        out_buf[j] = total.astype(BF16)
        stores.append(pltpu.make_async_copy(out_buf.at[j], outs[j], out_sems.at[j]))
        stores[-1].start()
    for store in stores:
        store.wait()


def sums(info, arrays, jobs):
    cols = arrays[0].shape[1]
    rows, terms = 128, sum(len(job) for job in jobs)
    return pl.pallas_call(
        functools.partial(sums_kernel, jobs, len(arrays)),
        grid_spec=pltpu.PrefetchScalarGridSpec(
            num_scalar_prefetch=1,
            grid=(1,),
            in_specs=[ANY] * len(arrays),
            out_specs=[ANY] * len(jobs),
            scratch_shapes=[
                pltpu.VMEM((terms, rows, cols), BF16),
                pltpu.VMEM((len(jobs), rows, cols), BF16),
                pltpu.SemaphoreType.DMA((terms,)),
                pltpu.SemaphoreType.DMA((len(jobs),)),
            ],
        ),
        out_shape=[shape_of((rows, cols), BF16)] * len(jobs),
        compiler_params=settings(1, 60),
        cost_estimate=cost(False),
        name="sums",
    )(info, *arrays)


def core_jobs(keep, came):
    return [[(a, far * 256, pick, False) for a in (keep, came)] for far in (0, 1) for pick in (0, 1)]


def core_sum_kernel(info, left_ref, right_ref, *outs):
    total = (left_ref[...].astype(F32) + right_ref[...].astype(F32)).astype(BF16)
    block = pl.program_id(1)
    place = block // 2 * 2 + jnp.bitwise_xor(block % 2, info[2])
    for i, out in enumerate(outs):

        @pl.when(place == i)
        def _():
            out[...] = total


def core_sum(info, keep, came):
    groups, rows, cols = keep.shape
    spec = pl.BlockSpec((1, rows // 4, cols), lambda g, i, info: (g, i, 0))
    return pl.pallas_call(
        core_sum_kernel,
        grid_spec=pltpu.PrefetchScalarGridSpec(
            num_scalar_prefetch=1,
            grid=(groups, 4),
            in_specs=[spec] * 2,
            out_specs=[pl.BlockSpec((1, rows // 4, cols), lambda g, i, info: (g, 0, 0))] * 4,
        ),
        out_shape=[shape_of((groups, rows // 4, cols), BF16)] * 4,
        compiler_params=settings(2, 24),
        cost_estimate=cost(False),
        name="core_sum",
    )(info, keep, came)


def weight_grad_kernel(nt_ref, back0_ref, back1_ref, gt_ref, att_ref, keep_ref, send_ref):
    cols = back0_ref.shape[2]
    part, block = pl.program_id(0), pl.program_id(1)

    def rows(target, back_ref):
        target[0, :, :cols] = dot(nt_ref[...], back_ref[0], 1, 0).astype(BF16)
        target[0, :, cols:] = dot(gt_ref[...], att_ref[0], 1, 0).astype(BF16)

    for j, back_ref in enumerate((back0_ref, back1_ref)):

        @pl.when((part == 0) & (block % 2 == j))
        def _():
            rows(send_ref, back_ref)

        @pl.when((part == 1) & (block % 2 == j))
        def _():
            rows(keep_ref, back_ref)


def weight_grad(normed_t, backs, grad_t, attended):
    width, tok = normed_t.shape
    cols, feats = backs[0].shape[2], attended.shape[2]
    half = pl.BlockSpec((width // 2, tok), lambda p, k: (1 - p, 0))
    side = pl.BlockSpec((1, tok, cols), lambda p, k: (k // 2, 0, 0))
    shape = (1, width // 2, cols + feats)
    return pl.pallas_call(
        weight_grad_kernel,
        grid=(2, 4),
        in_specs=[half, side, side, half, pl.BlockSpec((1, tok, feats), lambda p, k: (k, 0, 0))],
        out_specs=[
            pl.BlockSpec(shape, lambda p, k: (jnp.where(p == 0, 0, k), 0, 0)),
            pl.BlockSpec(shape, lambda p, k: (jnp.where(p == 0, k, 3), 0, 0)),
        ],
        out_shape=[shape_of((4, width // 2, cols + feats), BF16)] * 2,
        compiler_params=settings(2, 60),
        cost_estimate=cost(True),
        name="weight_grad",
    )(normed_t, *backs, grad_t, attended)


def copy_kernel(in_ref, out_ref):
    out_ref[...] = in_ref[...]


def copied(array):
    spec = pl.BlockSpec((1,) + array.shape[1:], lambda i: (i, 0, 0))
    return pl.pallas_call(
        copy_kernel,
        grid=(array.shape[0],),
        in_specs=[spec],
        out_specs=spec,
        out_shape=shape_of(array.shape, array.dtype),
        compiler_params=settings(1, 24),
        cost_estimate=cost(False),
        name="copied",
    )(array)


def after(value, *others):
    return lax.optimization_barrier((value,) + others)[0]


class Live:

    def update(self, **values):
        vars(self).update(values)


def per_device_rows(
    tokens,
    teacher,
    lengths,
    attn_gain,
    q_weight,
    k_weight,
    v_weight,
    q_gain,
    k_gain,
    o_weight,
    ffn_gain,
    gate_weight,
    up_weight,
    down_weight,
):
    z = lax.axis_index("tp")
    ctx = lax.axis_index("ctx")
    fsdp = lax.axis_index("fsdp")
    rows_dev, tok, width = tokens.shape
    quarter = width // 4
    hd = q_gain.shape[0] * 4
    q_cols, k_cols = q_weight.shape[1], k_weight.shape[1]
    proj = q_cols + 2 * k_cols
    heads = (q_cols // hd, k_cols // hd)
    units = gate_weight.shape[1]
    slots = rows_dev * 4 * tok * 2

    def x_swap(v):
        return lax.ppermute(v, "fsdp", X_SWAP)

    def core_swap(v):
        return lax.ppermute(v, "fsdp", CORE_SWAP)

    def y_swap(v):
        return lax.ppermute(v, "ctx", Y_SWAP)

    def z_up(v):
        return lax.ppermute(v, "tp", Z_UP)

    def z_far(v):
        return lax.ppermute(v, "tp", Z_FAR)

    def z_down(v):
        return lax.ppermute(v, "tp", Z_DOWN)

    def natural(v):
        v = jnp.concatenate([v[0:1], v[2:3], v[1:2], v[3:4]], axis=0)
        v = jnp.where(fsdp % 2 == 0, v, jnp.concatenate([v[1:2], v[0:1], v[3:4], v[2:3]], axis=0))
        return jnp.where(fsdp // 2 == 0, v, jnp.concatenate([v[2:4], v[0:2]], axis=0))

    v = Live()

    def sync():
        v.update(**lax.optimization_barrier(dict(vars(v))))

    length = lax.dynamic_slice_in_dim(lengths, z, 1, 0)
    info = jnp.concatenate([jnp.stack([z, fsdp, ctx]).astype(jnp.int32), length])
    w_proj = join(q_weight, k_weight, v_weight)
    proj_z = [z_up(w_proj), z_far(w_proj), z_down(w_proj)]
    proj_own = jnp.concatenate([w_proj, x_swap(w_proj)], axis=0)
    count_here = jnp.sum(lengths).astype(F32)[None]
    vector = jnp.concatenate([attn_gain, ffn_gain, q_gain, k_gain]).astype(F32)
    vector = jnp.concatenate([vector, count_here, jnp.zeros((640 - 545,), F32)])[None]
    vector = jnp.concatenate([vector, x_swap(vector)], axis=0)
    vector = jnp.concatenate([vector, core_swap(vector)], axis=0)
    w_out, w_ffn, *w_chunks = pack(info, o_weight, gate_weight, up_weight, down_weight)
    pos = (ctx * tok + jnp.arange(tok, dtype=jnp.int32)).astype(F32)
    frequency = THETA ** (-(2.0 * jnp.arange(hd // 2, dtype=F32)) / hd)
    angles = frequency[:, None] * pos[None, :]
    head_gains = natural(vector[:, 2 * quarter : 544])
    v.update(
        info=info,
        proj_own=proj_own,
        proj_z=jnp.concatenate(proj_z, axis=0),
        w_out=w_out,
        w_ffn=w_ffn,
        w_chunks=w_chunks,
        gain_one=vector[:, :quarter].reshape(1, width),
        gain_two=vector[:, quarter : 2 * quarter].reshape(1, width),
        total_count=jnp.sum(vector[:, 544]),
        gain_q=head_gains[:, : hd // 4].reshape(hd, 1),
        gain_k=head_gains[:, hd // 4 :].reshape(hd, 1),
        cos_part=jnp.cos(angles),
        sin_part=jnp.sin(angles),
    )
    sync()
    info = v.info

    proj_zfar = x_swap(v.proj_z)
    out_z = [z_up(v.w_out), z_far(v.w_out), z_down(v.w_out)]
    own_core = core_swap(v.proj_own)
    x_in, normed_one_t = norm_one(info, tokens, v.gain_one, 256)
    v.update(
        proj_zfar=proj_zfar, own_core=own_core, x_in=x_in, normed_one_t=normed_one_t, out_z=out_z
    )
    sync()

    plan_proj = [[(0, 0), (0, quarter), (3, 0), (3, quarter)]]
    plan_proj += [[(p, k * quarter) for p in (1, 2, 4, 5)] for k in range(3)]
    weights_proj = [v.proj_own, v.proj_z, v.proj_zfar, v.own_core]
    weights_proj += [core_swap(v.proj_z), core_swap(v.proj_zfar)]
    one = [z_up(v.w_chunks[0]), z_up(v.w_chunks[3])]
    ffn_far = x_swap(v.w_ffn)
    tables = [v.cos_part, v.sin_part, v.gain_q, v.gain_k]

    def make(block, *then):
        normed_t = after(v.normed_one_t, *then)
        return project(info, (plan_proj, weights_proj), normed_t, *tables, heads, block)

    theirs = [make(lambda s: 2 * (1 - s[2]))]
    got = [y_swap(theirs[0][0])]
    theirs.append(make(lambda s: 2 * (1 - s[2]) + 1, theirs[0][0]))
    got.append(y_swap(theirs[1][0]))
    mine = [make(lambda s: 2 * s[2], theirs[1][0])]
    mine.append(make(lambda s: 2 * s[2] + 1, mine[0][0]))
    v.update(
        one=one,
        ffn_far=ffn_far,
        weights_proj=weights_proj,
        mine=mine,
        theirs=theirs,
        got0=got[0],
    )
    sync()

    one_far = [x_swap(v.one[0])]
    three = [z_down(v.w_chunks[0])]
    own_cores = [core_swap(v.w_ffn), core_swap(v.ffn_far)]
    first = attn_fwd(info, v.mine[0][0], v.got0, hd)
    v.update(first=first, got1=got[1], one_far=one_far, three=three, own_cores=own_cores)
    sync()

    arrived = [y_swap(v.first[1])]
    three = v.three + [z_down(v.w_chunks[1])]
    out_blocks = jnp.concatenate([v.w_out] + v.out_z, axis=0)
    out_far = x_swap(out_blocks)
    one_cores = [core_swap(v.one[0]), core_swap(v.one_far[0])]
    second = attn_fwd(info, v.mine[1][0], v.got1, hd)
    v.update(
        second=second,
        arrived=arrived,
        three=three,
        out_blocks=out_blocks,
        out_far=out_far,
        one_cores=one_cores,
    )
    sync()

    arrived = v.arrived + [y_swap(v.second[1])]
    three = v.three + [z_down(v.w_chunks[2])]
    one_far = v.one_far + [x_swap(v.one[1][:, :units])]
    weights_out = [v.out_blocks, v.out_far]
    weights_out += [core_swap(v.out_blocks), core_swap(v.out_far)]
    v.update(arrived=arrived, three=three, one_far=one_far, weights_out=weights_out)
    sync()

    plan_out = [[(p, k * quarter) for p in range(4)] for k in range(4)]
    two = [z_up(v.one[0])]
    three_far = [x_swap(v.three[0])]
    one_far = v.one_far + [y_swap(v.one_far[0])]
    one_cores = v.one_cores + [core_swap(v.one[1]), core_swap(v.one_far[1])]
    resid, normed_two, normed_two_t, attended = out_proj(
        info,
        v.x_in,
        [v.first[0], v.second[0]],
        v.arrived,
        (plan_out, v.weights_out),
        v.gain_two,
        256,
    )
    v.update(
        two=two,
        three_far=three_far,
        one_far=one_far,
        one_cores=one_cores,
        resid=resid,
        normed_two=normed_two,
        normed_two_t=normed_two_t,
        attended=attended,
    )
    sync()

    plan0 = [[(i, 0, j * units) for j in range(3)] for i in range(4)]
    plan_mixed = [[(0, 0, 0), (1, 0, 0), (1, 0, units)], [(i, 0, 0) for i in (2, 3, 4)]]
    plan_mixed += [[(5, 0, 0), (6, 0, 0), (6, 0, units)], [(i, 0, 0) for i in (7, 8, 9)]]
    scale = (slots / v.total_count)[None]
    weights0 = [v.w_ffn, v.ffn_far] + v.own_cores
    c0, cf, c1, cb = v.one_cores
    weights1 = v.one + v.one_far + [c0, c1, cf, cb, core_swap(v.one_far[2])]
    two = v.two + [z_up(v.one[1])]
    three_far = v.three_far + [x_swap(v.three[1]), y_swap(v.three_far[0])]
    two_far = [x_swap(v.two[0])]
    three_cores = [core_swap(v.three[0])]
    acts_a, hiddens_a, sum_a = ffn_fwd(
        info,
        scale,
        v.normed_two,
        v.resid,
        None,
        [(plan0, weights0), (plan_mixed, weights1)],
        units,
        256,
    )
    v.update(
        scale=scale,
        weights0=weights0,
        weights1=weights1,
        two=two,
        three_far=three_far,
        two_far=two_far,
        three_cores=three_cores,
        acts_a=acts_a,
        hiddens_a=hiddens_a,
        sum_a=sum_a,
    )
    sync()

    plan_chunks = [[(3 * p + j, 0, 0) for j in range(3)] for p in range(4)]
    weights3 = v.three + v.three_far + v.three_cores
    weights3 += [core_swap(part) for part in v.three[1:]]
    weights3 += [core_swap(part) for part in v.three_far]
    two_far = v.two_far + [x_swap(v.two[1][:, :units]), y_swap(v.two_far[0])]
    two_cores = [core_swap(part) for part in v.two + v.two_far]
    acts_b, hiddens_b, sum_b = ffn_fwd(
        info, v.scale, v.normed_two, v.sum_a, None, [(plan_chunks, weights3)], units, 256
    )
    v.update(
        weights3=weights3,
        two_far=two_far,
        two_cores=two_cores,
        acts_b=acts_b,
        hiddens_b=hiddens_b,
        sum_b=sum_b,
    )
    sync()

    weights2 = v.two + v.two_far + v.two_cores
    weights2 += [core_swap(part) for part in v.two_far[1:]]
    acts_c, hiddens_c, result_low, grad_low, grad_low_t, square = ffn_fwd(
        info, v.scale, v.normed_two, v.sum_b, teacher, [(plan_mixed, weights2)], units, 256
    )
    v.update(
        weights2=weights2,
        acts_c=acts_c,
        hiddens_c=hiddens_c,
        result_low=result_low,
        grad_low=grad_low,
        grad_low_t=grad_low_t,
        square=square,
    )
    sync()

    def ffn_back(plan, weights, acts, hiddens, block, total):
        return ffn_bwd(
            v.grad_low,
            (acts, hiddens, block),
            (plan, weights),
            total,
            v.normed_two_t,
            v.grad_low_t,
            256,
        )

    turned = [False, False, True]
    output = lax.all_gather(v.result_low, "tp", axis=0, tiled=False)
    total, keep2, send2 = ffn_back(plan_mixed, v.weights2, v.acts_c, v.hiddens_c, 0, None)
    v.update(total=total, keep2=keep2, send2=send2)
    sync()

    came2 = core_swap(v.send2)
    total, keep1, send1 = ffn_back(plan_mixed, v.weights1, v.acts_a, v.hiddens_a, 1, v.total)
    v.update(came2=came2, total=total, keep1=keep1, send1=send1)
    sync()

    came1 = core_swap(v.send1)
    sum2 = sums(info, [v.keep2, v.came2], core_jobs(0, 1))
    far_t2 = x_swap(sum2[3])
    total, keep3, send3 = ffn_back(
        plan_chunks, v.weights3, v.acts_b, v.hiddens_b, 0, after(v.total, sum2[0])
    )
    v.update(
        came1=came1,
        sum2=sum2,
        far_t2=far_t2,
        total=total,
        keep3=keep3,
        send3=send3,
    )
    sync()

    came3 = core_swap(v.send3)
    far_h2 = x_swap(v.sum2[2])
    there2, *sum1 = sums(
        info,
        [v.sum2[1], v.far_t2, v.keep1, v.came1],
        [[(0, 0, None, False), (1, 0, None, False)]] + core_jobs(2, 3),
    )
    there2 = y_swap(there2)
    total, keep0, send0 = ffn_back(
        plan0, v.weights0, v.acts_a, v.hiddens_a, 0, after(v.total, sum1[0])
    )
    v.update(
        came3=came3,
        far_h2=far_h2,
        there2=there2,
        sum1=sum1,
        total=total,
        keep0=keep0,
        send0=send0,
    )
    sync()

    came0 = core_swap(v.send0)
    far_t1 = x_swap(v.sum1[3])
    plane = [(0, 0, None, False), (1, 0, None, False), (2, 0, None, True)]
    part2, *sum3 = sums(
        info,
        [v.sum2[0], v.far_h2, v.there2, v.keep3, v.came3],
        [plane] + core_jobs(3, 4),
    )
    down2 = z_down(part2)
    grad_resid, grad_attn_t, a0, a1, b0, b1, gain_two_sum = norm_two_back(
        info,
        after(v.total, sum3[0]),
        v.resid,
        v.grad_low,
        v.gain_two,
        (plan_out, v.weights_out),
        256,
    )
    grad_got = [y_swap(b0), y_swap(b1)]
    v.update(
        came0=came0,
        far_t1=far_t1,
        sum3=sum3,
        grad_resid=grad_resid,
        grad_attn_t=grad_attn_t,
        grad_mine=[a0, a1],
        gain_two_sum=gain_two_sum,
    )
    sync()

    def attn_back(j, grad):
        out = (v.first, v.second)[j]
        got_ref = (v.got0, v.got1)[j]
        arrived = (v.grad_got0, grad_got[1] if j == 0 else v.grad_got1)[j]
        return attn_bwd(
            info, v.mine[j][0], got_ref, out[0], out[1], grad, arrived, out[2], hd
        )

    far_h1 = x_swap(v.sum1[2])
    there1, *sum0 = sums(
        info,
        [v.sum1[1], v.far_t1, v.keep0, v.came0],
        [[(0, 0, None, False), (1, 0, None, False)]] + core_jobs(2, 3),
    )
    there1 = y_swap(there1)
    far_t3 = x_swap(v.sum3[3])
    v.update(grad_got0=grad_got[0])
    back0 = attn_back(0, after(v.grad_mine[0], sum0[0]))
    v.update(
        far_h1=far_h1,
        there1=there1,
        far_t3=far_t3,
        down2=down2,
        sum0=sum0,
        back0=back0,
        grad_got1=grad_got[1],
    )
    sync()

    heads0 = y_swap(v.back0[1])
    far_h3 = x_swap(v.sum3[2])
    far_t0 = x_swap(v.sum0[3])
    there3, two_down = sums(
        info,
        [v.sum3[1], v.far_t3, v.sum1[0], v.far_h1, v.there1, v.down2],
        [
            [(0, 0, None, False), (1, 0, None, False)],
            [(2, 0, None, False), (3, 0, None, False), (4, 0, None, True), (5, 0, None, False)],
        ],
    )
    there3_got = y_swap(there3)
    two_down_got = z_down(two_down)
    back1 = attn_back(1, after(v.grad_mine[1], there3, two_down, output))
    v.update(
        heads0=heads0, far_h3=far_h3, far_t0=far_t0, there3=there3_got, back1=back1
    )
    sync()

    heads1 = y_swap(v.back1[1])
    far_h0 = x_swap(v.sum0[2])
    part3, there0 = sums(
        info,
        [v.sum3[0], v.far_h3, v.there3, v.sum0[1], v.far_t0],
        [plane, [(3, 0, None, False), (4, 0, None, False)]],
    )
    up3 = z_up(part3)
    tables = [v.cos_part, v.sin_part, v.gain_q, v.gain_k]
    head0 = head_back(
        info, v.back0[0], v.heads0, v.mine[0][1], v.theirs[0][1], *tables, heads
    )
    v.update(heads1=heads1, head0=head0, there0=there0)
    sync()

    there0 = y_swap(v.there0)
    head1 = head_back(
        info, v.back1[0], v.heads1, v.mine[1][1], v.theirs[1][1], *tables, heads
    )
    def last_norm(part, *then):
        return norm_one_back(
            info,
            [v.head0[0], after(head1[0], *then)],
            (plan_proj, v.weights_proj),
            v.x_in,
            v.grad_resid,
            v.gain_one,
            tok // 4,
            part,
        )

    low_first, gain_first = last_norm(0)
    low_second, gain_second = last_norm(1, low_first)
    gathered = [lax.all_gather(low_first, "tp", axis=0, tiled=False)]
    tokens_low, gain_one_sum = low_second, gain_first + gain_second
    v.update(head1=head1, tokens_low=tokens_low, gain_one_sum=gain_one_sum, up3=up3)
    v.update(there0=there0, far_h0=far_h0, two_down=two_down_got)
    sync()

    gathered.append(lax.all_gather(v.tokens_low, "tp", axis=0, tiled=False))
    keep, send = weight_grad(
        v.normed_one_t, [v.head0[0], v.head1[0]], v.grad_attn_t, v.attended
    )
    gain_heads = v.head0[1] + v.head1[1]
    vector = jnp.concatenate(
        [
            natural(v.gain_one_sum.reshape(4, quarter)).reshape(1, width),
            natural(v.gain_two_sum.reshape(4, quarter)).reshape(1, width),
            gain_heads[:, 0].reshape(1, hd),
            gain_heads[:, 1].reshape(1, hd),
            jnp.sum(v.square).reshape(1, 1),
            jnp.zeros((1, 127), F32),
        ],
        axis=1,
    )
    vector = vector + core_swap(vector)
    v.update(keep=keep, send=send)
    v.update(vector=vector)
    sync()

    rows = quarter // 2
    flat = lambda a: a.reshape(4 * rows, a.shape[-1])
    attn_sums = [flat(p) for p in core_sum(info, v.keep, core_swap(v.send))]
    vector = v.vector + x_swap(v.vector)
    v.update(sums=attn_sums, vector=vector)
    sync()

    far_t = x_swap(v.sums[3])
    part0 = summed([v.sum0[0], v.far_h0, v.there0], turned)
    ffn_sum = summed([part0, v.two_down, v.up3], None, F32)
    vector = v.vector + y_swap(v.vector)
    v.update(far_t=far_t, ffn_sum=ffn_sum, vector=vector)
    sync()

    far_h = x_swap(v.sums[2])
    there = y_swap(summed([v.sums[1], v.far_t]))
    spread = copied(output)
    v.update(far_h=far_h, there=there, spread=spread)
    sync()

    parts = summed([v.sums[0], v.far_h, v.there])
    parts = [parts[k * rows : (k + 1) * rows] for k in range(4)]
    parts = [parts[0], z_down(parts[1]), z_far(parts[2]), z_up(parts[3])]
    ffn_other = y_swap(v.ffn_sum)
    v.update(parts=parts)
    sync()

    attn_sum = summed(v.parts, None, F32)
    vector = v.vector + lax.ppermute(v.vector, "tp", Z_NEAR)
    v.update(attn_sum=attn_sum, vector=vector)
    v.update(ffn_other=ffn_other)
    sync()

    def finish(own, other):
        return jnp.concatenate(
            [jnp.where(ctx == 0, own, other), jnp.where(ctx == 0, other, own)], axis=0
        )

    def columns(first):
        parts = [ffn_grad[:, first(j) : first(j) + third] for j in range(3)]
        return jnp.concatenate(
            [
                jnp.where(ctx == 0, parts[0], parts[2]),
                parts[1],
                jnp.where(ctx == 0, parts[2], parts[0]),
            ],
            axis=1,
        )

    attn_other = y_swap(v.attn_sum)
    vector = v.vector + lax.ppermute(v.vector, "tp", Z_FAR)
    third = units // 3
    ffn_grad = finish(v.ffn_sum, turn_chunks(v.ffn_other))
    grad_gate = columns(lambda j: 2 * j * third)
    grad_up = columns(lambda j: (2 * j + 1) * third)
    grad_down = columns(lambda j: 2 * units + j * third).T
    grad = jnp.zeros((rows_dev, tok, width), F32)
    grad = lax.dynamic_update_slice(grad, gathered[0].astype(F32), (0, 0, 0))
    v.update(vector=vector, attn_other=attn_other, grad=grad)
    v.update(grad_gate=grad_gate, grad_up=grad_up, grad_down=grad_down)
    sync()

    tokens_grad = lax.dynamic_update_slice(v.grad, gathered[1].astype(F32), (0, tok // 2, 0))
    sums_all = v.vector[0]

    attn_grad = finish(v.attn_sum, v.attn_other)
    teacher_loss = sums_all[2 * width + 2 * hd] / (v.total_count * width)

    def own_part(at, size):
        return lax.dynamic_slice_in_dim(sums_all, at + fsdp * (size // 4), size // 4, 0)

    return (
        v.spread,
        teacher_loss,
        tokens_grad,
        own_part(0, width),
        attn_grad[:, :q_cols],
        attn_grad[:, q_cols : q_cols + k_cols],
        attn_grad[:, q_cols + k_cols : proj],
        own_part(2 * width, hd),
        own_part(2 * width + hd, hd),
        attn_grad[:, proj:].T,
        own_part(width, width),
        v.grad_gate,
        v.grad_up,
        v.grad_down,
    )


def solution(mesh):
    return jax.shard_map(
        per_device_rows if fits(mesh) else per_device_any,
        mesh=mesh,
        in_specs=(
            P("fsdp", "ctx", None),
            P("fsdp", "ctx", None),
            P("fsdp"),
            P("fsdp"),
            P("fsdp", "tp"),
            P("fsdp", "tp"),
            P("fsdp", "tp"),
            P("fsdp"),
            P("fsdp"),
            P("tp", "fsdp"),
            P("fsdp"),
            P("fsdp", "tp"),
            P("fsdp", "tp"),
            P("tp", "fsdp"),
        ),
        out_specs=(
            P("fsdp", "ctx", None),
            P(),
            P("fsdp", "ctx", None),
            P("fsdp"),
            P("fsdp", "tp"),
            P("fsdp", "tp"),
            P("fsdp", "tp"),
            P("fsdp"),
            P("fsdp"),
            P("tp", "fsdp"),
            P("fsdp"),
            P("fsdp", "tp"),
            P("fsdp", "tp"),
            P("tp", "fsdp"),
        ),
        check_vma=False,
    )
```

```python
import functools
import math

import jax
import jax.numpy as jnp
from jax import lax
from jax.experimental import pallas as pl
from jax.experimental.pallas import tpu as pltpu
from jax.sharding import PartitionSpec as P

EPS = 1e-05
THETA = 1000000.0
NEGATIVE = -1e30


def rms_scale(field_in, gain_vec):
    return (
        field_in * lax.rsqrt(jnp.mean(field_in * field_in, axis=-1, keepdims=True) + EPS) * gain_vec
    )


def rotate(field_in, positions):
    half_dim = field_in.shape[-1] // 2
    frequency = THETA ** (-(2.0 * jnp.arange(half_dim, dtype=jnp.float32)) / field_in.shape[-1])
    angles = positions[:, None] * frequency[None, :]
    cos_part = jnp.cos(angles)[:, None, :]
    sin_part = jnp.sin(angles)[:, None, :]
    lower_half = field_in[..., :half_dim]
    upper_half = field_in[..., half_dim:]
    return jnp.concatenate(
        [
            lower_half * cos_part - upper_half * sin_part,
            upper_half * cos_part + lower_half * sin_part,
        ],
        axis=-1,
    )


def linear(left_mat, right_mat):
    return jnp.dot(left_mat, right_mat, preferred_element_type=jnp.float32)


def linear_left(left_mat, right_mat):
    return lax.dot_general(
        left_mat, right_mat, (((0,), (0,)), ((), ())), preferred_element_type=jnp.float32
    )


def linear_right(left_mat, right_mat):
    return lax.dot_general(
        left_mat, right_mat, (((1,), (1,)), ((), ())), preferred_element_type=jnp.float32
    )


def swiglu(gate_act, up_act):
    return jax.nn.silu(gate_act) * up_act


def per_device_any(
    tokens,
    teacher,
    lengths,
    attn_gain,
    q_weight,
    k_weight,
    v_weight,
    q_gain,
    k_gain,
    o_weight,
    ffn_gain,
    gate_weight,
    up_weight,
    down_weight,
):
    (
        gain_one,
        w_query,
        w_key,
        w_value,
        gain_query,
        gain_key,
        w_output,
        gain_two,
        w_gate,
        w_upper,
        w_down,
    ) = (
        lax.all_gather(attn_gain, "fsdp", axis=0, tiled=True),
        lax.all_gather(q_weight, "fsdp", axis=0, tiled=True),
        lax.all_gather(k_weight, "fsdp", axis=0, tiled=True),
        lax.all_gather(v_weight, "fsdp", axis=0, tiled=True),
        lax.all_gather(q_gain, "fsdp", axis=0, tiled=True),
        lax.all_gather(k_gain, "fsdp", axis=0, tiled=True),
        lax.all_gather(o_weight, "fsdp", axis=1, tiled=True),
        lax.all_gather(ffn_gain, "fsdp", axis=0, tiled=True),
        lax.all_gather(gate_weight, "fsdp", axis=0, tiled=True),
        lax.all_gather(up_weight, "fsdp", axis=0, tiled=True),
        lax.all_gather(down_weight, "fsdp", axis=1, tiled=True),
    )
    rows_dev, block_len, model_width = tokens.shape
    count_tok = rows_dev * block_len
    head_dim = gain_query.shape[0]
    q_heads = w_query.shape[1] // head_dim
    kv_heads = w_key.shape[1] // head_dim
    group_size = q_heads // kv_heads
    score_scale = head_dim ** (-0.5)
    row_len = block_len * lax.axis_size("ctx")
    key_block = math.gcd(row_len, 512)
    block_start = lax.axis_index("ctx") * block_len
    tiles_used = (block_start + block_len + key_block - 1) // key_block
    slot_pos = block_start + jnp.arange(block_len, dtype=jnp.int32)
    positions = slot_pos.astype(jnp.float32)
    valid = (slot_pos[None, :] < lengths[:, None]).astype(jnp.float32)
    slots = count_tok * lax.axis_size("fsdp") * lax.axis_size("ctx")
    gain_two_f = gain_two.astype(jnp.float32)
    gain_one_f = gain_one.astype(jnp.float32)
    inputs = tokens.astype(jnp.float32)
    normed_one, back_one = jax.vjp(rms_scale, inputs, gain_one_f)
    normed_low = normed_one.astype(jnp.bfloat16).reshape(count_tok, model_width)
    query_raw = linear(normed_low, w_query)
    key_raw = linear(normed_low, w_key)
    value_raw = linear(normed_low, w_value)

    def heads_post(raw_heads, gain_vec):
        shaped = raw_heads.reshape(rows_dev, block_len, -1, head_dim)
        return rotate(rms_scale(shaped, gain_vec), positions)

    query_rot, query_back = jax.vjp(heads_post, query_raw, gain_query.astype(jnp.float32))
    key_rot, key_back = jax.vjp(heads_post, key_raw, gain_key.astype(jnp.float32))
    queries = query_rot.astype(jnp.bfloat16).reshape(
        rows_dev, block_len, kv_heads, group_size, head_dim
    )
    key_rows = key_rot.astype(jnp.bfloat16).reshape(rows_dev, block_len, kv_heads * head_dim)
    values = value_raw.astype(jnp.bfloat16).reshape(rows_dev, block_len, kv_heads * head_dim)
    keys_all, values_all = (
        lax.all_gather(key_rows, "ctx", axis=1, tiled=True),
        lax.all_gather(values, "ctx", axis=1, tiled=True),
    )

    def key_tile(tile_index):
        tile_start = tile_index * key_block
        key_pos = tile_start + jnp.arange(key_block, dtype=jnp.int32)
        key_part = lax.dynamic_slice_in_dim(keys_all, tile_start, key_block, 1).reshape(
            rows_dev, key_block, kv_heads, head_dim
        )
        value_part = lax.dynamic_slice_in_dim(values_all, tile_start, key_block, 1).reshape(
            rows_dev, key_block, kv_heads, head_dim
        )
        scores = (
            jnp.einsum("rqhgd,rkhd->rhgqk", queries, key_part, preferred_element_type=jnp.float32)
            * score_scale
        )
        allowed = (key_pos[None, None, :] <= slot_pos[None, :, None]) & (
            key_pos[None, None, :] < lengths[:, None, None]
        )
        return (tile_start, scores, allowed[:, None, None], key_part, value_part)

    stat_shape = (rows_dev, kv_heads, group_size, block_len)

    def stats_step(tile_index, carried):
        running_max, running_sum = carried
        tile_start, scores, allowed, key_part, value_part = key_tile(tile_index)
        masked = jnp.where(allowed, scores, NEGATIVE)
        new_max = jnp.maximum(running_max, jnp.max(masked, axis=-1))
        terms = jnp.where(allowed, jnp.exp(masked - new_max[..., None]), 0.0)
        return (new_max, running_sum * jnp.exp(running_max - new_max) + jnp.sum(terms, axis=-1))

    running_max, running_sum = lax.fori_loop(
        0,
        tiles_used,
        stats_step,
        (jnp.full(stat_shape, NEGATIVE, jnp.float32), jnp.zeros(stat_shape, jnp.float32)),
    )
    log_total = running_max + jnp.log(running_sum)
    out_shape = (rows_dev, block_len, kv_heads, group_size, head_dim)

    def value_step(tile_index, carried):
        rounded_out, exact_out = carried
        tile_start, scores, allowed, key_part, value_part = key_tile(tile_index)
        tile_probs = jnp.where(allowed, jnp.exp(scores - log_total[..., None]), 0.0)
        rounded_out = rounded_out + jnp.einsum(
            "rhgqk,rkhd->rqhgd",
            tile_probs.astype(jnp.bfloat16),
            value_part,
            preferred_element_type=jnp.float32,
        )
        exact_out = exact_out + jnp.einsum(
            "rhgqk,rkhd->rqhgd", tile_probs, value_part.astype(jnp.float32)
        )
        return (rounded_out, exact_out)

    rounded_out, exact_out = lax.fori_loop(
        0,
        tiles_used,
        value_step,
        (jnp.zeros(out_shape, jnp.float32), jnp.zeros(out_shape, jnp.float32)),
    )
    attended = rounded_out.astype(jnp.bfloat16).reshape(count_tok, q_heads * head_dim)
    attn_total = lax.psum(linear(attended, w_output), "tp")
    resid = inputs + attn_total.reshape(rows_dev, block_len, model_width)
    normed_two, back_two = jax.vjp(rms_scale, resid, gain_two_f)
    normed_second = normed_two.astype(jnp.bfloat16).reshape(count_tok, model_width)
    gate_act = linear(normed_second, w_gate)
    up_act = linear(normed_second, w_upper)
    hidden_full, back_glu = jax.vjp(swiglu, gate_act, up_act)
    hidden = hidden_full.astype(jnp.bfloat16)
    ffn_total = lax.psum(linear(hidden, w_down), "tp")
    result = resid + ffn_total.reshape(rows_dev, block_len, model_width)
    error_value = result - teacher.astype(jnp.float32)
    valid_col = valid[..., None]
    total_square, total_count = lax.psum(
        (jnp.sum(valid_col * error_value * error_value), jnp.sum(valid)), ("fsdp", "ctx")
    )
    teacher_loss = total_square / (total_count * model_width)
    grad_result = valid_col * error_value * (slots / total_count)
    grad_low = grad_result.astype(jnp.bfloat16).reshape(count_tok, model_width)
    grad_down = linear_left(hidden, grad_low)
    grad_hidden = linear_right(grad_low, w_down)
    grad_gate_full, grad_up_full = back_glu(grad_hidden)
    grad_gate = grad_gate_full.astype(jnp.bfloat16)
    grad_up = grad_up_full.astype(jnp.bfloat16)
    grad_wgate = linear_left(normed_second, grad_gate)
    grad_wup = linear_left(normed_second, grad_up)
    normed_two_part = linear_right(grad_gate, w_gate) + linear_right(grad_up, w_upper)
    grad_normed_two = lax.psum(normed_two_part, "tp")
    grad_resid_norm, grad_gain_two = back_two(
        grad_normed_two.reshape(rows_dev, block_len, model_width)
    )
    grad_resid = grad_result + grad_resid_norm
    grad_attn_low = grad_resid.astype(jnp.bfloat16).reshape(count_tok, model_width)
    grad_woutput = linear_left(attended, grad_attn_low)
    grad_attended = linear_right(grad_attn_low, w_output).astype(jnp.bfloat16).reshape(out_shape)
    delta = jnp.einsum("rqhgd,rqhgd->rhgq", grad_attended.astype(jnp.float32), exact_out)
    full_shape = (rows_dev, row_len, kv_heads * head_dim)

    def grad_step(tile_index, carried):
        grad_queries, grad_keys, grad_values = carried
        tile_start, scores, allowed, key_part, value_part = key_tile(tile_index)
        tile_probs = jnp.where(allowed, jnp.exp(scores - log_total[..., None]), 0.0)
        grad_probs = jnp.einsum(
            "rqhgd,rkhd->rhgqk", grad_attended, value_part, preferred_element_type=jnp.float32
        )
        grad_scores = (tile_probs * (grad_probs - delta[..., None])).astype(jnp.bfloat16)
        grad_queries = (
            grad_queries
            + jnp.einsum(
                "rhgqk,rkhd->rqhgd", grad_scores, key_part, preferred_element_type=jnp.float32
            )
            * score_scale
        )
        key_term = (
            jnp.einsum(
                "rhgqk,rqhgd->rkhd", grad_scores, queries, preferred_element_type=jnp.float32
            )
            * score_scale
        )
        value_term = jnp.einsum(
            "rhgqk,rqhgd->rkhd",
            tile_probs.astype(jnp.bfloat16),
            grad_attended,
            preferred_element_type=jnp.float32,
        )
        grad_keys = lax.dynamic_update_slice_in_dim(
            grad_keys, key_term.reshape(rows_dev, key_block, kv_heads * head_dim), tile_start, 1
        )
        grad_values = lax.dynamic_update_slice_in_dim(
            grad_values, value_term.reshape(rows_dev, key_block, kv_heads * head_dim), tile_start, 1
        )
        return (grad_queries, grad_keys, grad_values)

    grad_queries, grad_keys, grad_values = lax.fori_loop(
        0,
        tiles_used,
        grad_step,
        (
            jnp.zeros(out_shape, jnp.float32),
            jnp.zeros(full_shape, jnp.float32),
            jnp.zeros(full_shape, jnp.float32),
        ),
    )
    key_grad, value_grad = (
        lax.psum_scatter(grad_keys, "ctx", scatter_dimension=1, tiled=True),
        lax.psum_scatter(grad_values, "ctx", scatter_dimension=1, tiled=True),
    )
    grad_query_raw, grad_gain_query = query_back(
        grad_queries.reshape(rows_dev, block_len, q_heads, head_dim)
    )
    grad_key_raw, grad_gain_key = key_back(
        key_grad.reshape(rows_dev, block_len, kv_heads, head_dim)
    )
    query_low = grad_query_raw.astype(jnp.bfloat16)
    key_low = grad_key_raw.astype(jnp.bfloat16)
    value_low = value_grad.reshape(count_tok, kv_heads * head_dim).astype(jnp.bfloat16)
    grad_wquery = linear_left(normed_low, query_low)
    grad_wkey = linear_left(normed_low, key_low)
    grad_wvalue = linear_left(normed_low, value_low)
    normed_part = (
        linear_right(query_low, w_query)
        + linear_right(key_low, w_key)
        + linear_right(value_low, w_value)
    )
    grad_normed_one, grad_gain_query, grad_gain_key = lax.psum(
        (normed_part, grad_gain_query, grad_gain_key), "tp"
    )
    grad_input_norm, grad_gain_one = back_one(
        grad_normed_one.reshape(rows_dev, block_len, model_width)
    )
    tokens_grad = grad_resid + grad_input_norm
    partials = (
        grad_gain_one,
        grad_wquery,
        grad_wkey,
        grad_wvalue,
        grad_gain_query,
        grad_gain_key,
        grad_woutput,
        grad_gain_two,
        grad_wgate,
        grad_wup,
        grad_down,
    )
    pieces = (
        lax.psum_scatter(partials[0], ("fsdp", "ctx"), scatter_dimension=0, tiled=True),
        lax.psum_scatter(partials[1], ("fsdp", "ctx"), scatter_dimension=0, tiled=True),
        lax.psum_scatter(partials[2], ("fsdp", "ctx"), scatter_dimension=0, tiled=True),
        lax.psum_scatter(partials[3], ("fsdp", "ctx"), scatter_dimension=0, tiled=True),
        lax.psum_scatter(partials[4], ("fsdp", "ctx"), scatter_dimension=0, tiled=True),
        lax.psum_scatter(partials[5], ("fsdp", "ctx"), scatter_dimension=0, tiled=True),
        lax.psum_scatter(partials[6], ("fsdp", "ctx"), scatter_dimension=1, tiled=True),
        lax.psum_scatter(partials[7], ("fsdp", "ctx"), scatter_dimension=0, tiled=True),
        lax.psum_scatter(partials[8], ("fsdp", "ctx"), scatter_dimension=0, tiled=True),
        lax.psum_scatter(partials[9], ("fsdp", "ctx"), scatter_dimension=0, tiled=True),
        lax.psum_scatter(partials[10], ("fsdp", "ctx"), scatter_dimension=1, tiled=True),
    )
    summed = (
        lax.all_gather(pieces[0], "ctx", axis=0, tiled=True),
        lax.all_gather(pieces[1], "ctx", axis=0, tiled=True),
        lax.all_gather(pieces[2], "ctx", axis=0, tiled=True),
        lax.all_gather(pieces[3], "ctx", axis=0, tiled=True),
        lax.all_gather(pieces[4], "ctx", axis=0, tiled=True),
        lax.all_gather(pieces[5], "ctx", axis=0, tiled=True),
        lax.all_gather(pieces[6], "ctx", axis=1, tiled=True),
        lax.all_gather(pieces[7], "ctx", axis=0, tiled=True),
        lax.all_gather(pieces[8], "ctx", axis=0, tiled=True),
        lax.all_gather(pieces[9], "ctx", axis=0, tiled=True),
        lax.all_gather(pieces[10], "ctx", axis=1, tiled=True),
    )
    return (
        result.astype(jnp.bfloat16),
        teacher_loss,
        tokens_grad,
        summed[0],
        summed[1],
        summed[2],
        summed[3],
        summed[4],
        summed[5],
        summed[6],
        summed[7],
        summed[8],
        summed[9],
        summed[10],
    )


BF16 = jnp.bfloat16
F32 = jnp.float32
LOG2E = math.log2(math.e)
X_SWAP = [(0, 2), (2, 0), (1, 3), (3, 1)]
CORE_SWAP = [(0, 1), (1, 0), (2, 3), (3, 2)]
Y_SWAP = [(0, 1), (1, 0)]
Z_UP = [(0, 1), (1, 2), (2, 3), (3, 0)]
Z_DOWN = [(0, 3), (1, 0), (2, 1), (3, 2)]
Z_NEAR = [(0, 1), (1, 0), (2, 3), (3, 2)]
Z_FAR = [(0, 2), (2, 0), (1, 3), (3, 1)]
MASKS = (0, 2, 1, 3)
ANY = pl.BlockSpec(memory_space=pl.ANY)
SMEM = pl.BlockSpec(memory_space=pltpu.SMEM)


def fits(mesh):
    return dict(mesh.shape) == {"fsdp": 4, "ctx": 2, "tp": 4}


def dot(left, right, left_dim, right_dim):
    return lax.dot_general(
        left, right, (((left_dim,), (right_dim,)), ((), ())), preferred_element_type=F32
    )


def sigmoid(v):
    return 0.5 * jnp.tanh(0.5 * v) + 0.5


def whole(shape):
    zeros = (0,) * len(shape)
    return pl.BlockSpec(shape, lambda *_: zeros, pipeline_mode=pl.Buffered(1))


def settings(dims, mib):
    return pltpu.CompilerParams(
        dimension_semantics=("arbitrary",) * dims, vmem_limit_bytes=mib << 20
    )


def shape_of(shape, dtype):
    return jax.ShapeDtypeStruct(shape, dtype)


def cost(large, microseconds=None):
    size = 1 << 42 if large else 1 << 10
    if microseconds is not None:
        size = int(microseconds * 1.15e9)
    return pl.CostEstimate(flops=size, bytes_accessed=size >> 12, transcendentals=0)


def pack_kernel(info, o_in, g_in, u_in, d_in, *refs):
    out_ref, ffn_ref, *chunk_refs, others_ref, o_ref, g_ref, u_ref, d_ref, sems = refs
    ctx = info[2]
    pairs = ((o_in, o_ref), (g_in, g_ref), (u_in, u_ref), (d_in, d_ref))
    copies = [pltpu.make_async_copy(a, b, sems.at[i]) for i, (a, b) in enumerate(pairs)]
    for copy in copies:
        copy.start()
    for copy in copies:
        copy.wait()
    out_ref[...] = o_ref[...].astype(F32).T.astype(BF16)
    third = g_ref.shape[1] // 3
    for j in range(3):
        at = pl.multiple_of(jnp.where(ctx == 0, j, 2 - j) * third, third)
        parts = [
            g_ref[:, pl.ds(at, third)],
            u_ref[:, pl.ds(at, third)],
            d_ref[pl.ds(at, third), :].astype(F32).T.astype(BF16),
        ]
        for i, part in enumerate(parts):
            chunk_refs[j][:, i * third : (i + 1) * third] = part
            if j:
                others_ref[:, (3 * j - 3 + i) * third : (3 * j - 2 + i) * third] = part
            ffn_ref[:, (3 * j + i) * third : (3 * j + i + 1) * third] = part


def pack(info, o, g, u, d):
    rows, units = g.shape
    feats = o.shape[0]
    widths = (feats, 3 * units, units, units, units, 2 * units)
    return pl.pallas_call(
        pack_kernel,
        in_specs=[SMEM] + [ANY] * 4,
        out_specs=[pl.BlockSpec(memory_space=pltpu.VMEM)] * 6,
        out_shape=[shape_of((rows, n), BF16) for n in widths],
        scratch_shapes=[pltpu.VMEM(a.shape, BF16) for a in (o, g, u, d)]
        + [pltpu.SemaphoreType.DMA((4,))],
        compiler_params=pltpu.CompilerParams(vmem_limit_bytes=24 << 20),
        cost_estimate=cost(False),
        name="pack",
    )(info, o, g, u, d)


def join_kernel(q_ref, k_ref, v_ref, out_ref):
    at = 0
    for ref in (q_ref, k_ref, v_ref):
        out_ref[:, at : at + ref.shape[1]] = ref[...]
        at += ref.shape[1]


def join(q, k, v):
    return pl.pallas_call(
        join_kernel,
        out_shape=shape_of((q.shape[0], q.shape[1] + k.shape[1] + v.shape[1]), BF16),
        compiler_params=pltpu.CompilerParams(vmem_limit_bytes=8 << 20),
        cost_estimate=cost(False),
        name="join",
    )(q, k, v)


def norm_one_kernel(info, tok_ref, gain_ref, x_ref, nt_ref, x32):
    quarter = x_ref.shape[1] // 4
    for p, mask in enumerate(MASKS):
        at = pl.multiple_of(jnp.bitwise_xor(info[1], mask) * quarter, quarter)
        part = tok_ref[0, :, pl.ds(at, quarter)]
        x_ref[:, p * quarter : (p + 1) * quarter] = part
        x32[:, p * quarter : (p + 1) * quarter] = part.astype(F32)
    x = x32[...]
    rho = lax.rsqrt(jnp.mean(x * x, axis=-1, keepdims=True) + EPS)
    nt_ref[...] = (x * rho * gain_ref[...]).T.astype(BF16)


def norm_one(info, tokens, gain, tile):
    _, tok, width = tokens.shape
    return pl.pallas_call(
        norm_one_kernel,
        grid_spec=pltpu.PrefetchScalarGridSpec(
            num_scalar_prefetch=1,
            grid=(tok // tile,),
            in_specs=[
                pl.BlockSpec((1, tile, width), lambda i, info: (info[0], i, 0)),
                pl.BlockSpec((1, width), lambda i, info: (0, 0)),
            ],
            out_specs=[
                pl.BlockSpec((tile, width), lambda i, info: (i, 0)),
                pl.BlockSpec((width, tile), lambda i, info: (0, i)),
            ],
            scratch_shapes=[pltpu.VMEM((tile, width), F32)],
        ),
        out_shape=[shape_of((tok, width), BF16), shape_of((width, tok), BF16)],
        compiler_params=settings(1, 24),
        cost_estimate=cost(False),
        name="norm_one",
    )(info, tokens, gain)


def proj_kernel(heads, block, plan, count, info, *refs):
    nt_ref, cos_ref, sin_ref, qg_ref, kg_ref, rot_ref, raw_ref, w_ref, sem = refs[count:]
    rows = w_ref.shape[0] // 4

    @pl.when(pl.program_id(0) == 0)
    def _():
        for k in range(4):

            @pl.when(block(info) == k)
            def _():
                for p, (piece, row) in enumerate(plan[k]):
                    src = refs[piece].at[pl.ds(row, rows)]
                    pltpu.make_async_copy(src, w_ref.at[pl.ds(p * rows, rows)], sem).start()

        pltpu.make_async_copy(w_ref, w_ref, sem).wait()

    hd = qg_ref.shape[0]
    half = hd // 2
    raw = dot(w_ref[...], nt_ref[...], 0, 0)
    cos_part, sin_part = cos_ref[...], sin_ref[...]
    heads_q, heads_k = heads
    raw_ref[...] = raw.astype(BF16)
    for h in range(heads_q + heads_k):
        v = raw[h * hd : (h + 1) * hd]
        rho = lax.rsqrt(jnp.mean(v * v, axis=0, keepdims=True) + EPS)
        v = v * rho * (qg_ref[...] if h < heads_q else kg_ref[...])
        a, b = v[:half], v[half:]
        rot_ref[h * hd : h * hd + half, :] = (a * cos_part - b * sin_part).astype(BF16)
        rot_ref[h * hd + half : (h + 1) * hd, :] = (b * cos_part + a * sin_part).astype(BF16)
    at = (heads_q + heads_k) * hd
    rot_ref[at:, :] = raw[at:].astype(BF16)


def project(info, weights, normed_t, cos_part, sin_part, gain_q, gain_k, heads, block):
    plan, pieces = weights
    width, tok = normed_t.shape
    cols = pieces[0].shape[1]
    tile = min(512, tok)
    const = lambda a: pl.BlockSpec(a.shape, lambda i, info: (0, 0))
    tab = lambda a: pl.BlockSpec((a.shape[0], tile), lambda i, info: (0, i))
    return pl.pallas_call(
        functools.partial(proj_kernel, heads, block, plan, len(pieces)),
        grid_spec=pltpu.PrefetchScalarGridSpec(
            num_scalar_prefetch=1,
            grid=(tok // tile,),
            in_specs=[ANY] * len(pieces)
            + [tab(normed_t), tab(cos_part), tab(sin_part), const(gain_q), const(gain_k)],
            out_specs=[pl.BlockSpec((cols, tile), lambda i, info: (0, i))] * 2,
            scratch_shapes=[pltpu.VMEM((width, cols), BF16), pltpu.SemaphoreType.DMA],
        ),
        out_shape=[shape_of((cols, tok), BF16), shape_of((cols, tok), BF16)],
        compiler_params=settings(1, 24),
        cost_estimate=cost(False),
        name="project",
    )(info, *pieces, normed_t, cos_part, sin_part, gain_q, gain_k)


def head_back_kernel(
    heads, info, dm_ref, dt_ref, rm_ref, rt_ref, cos_ref, sin_ref, qg_ref, kg_ref, out_ref, gg_ref
):
    step, part = pl.program_id(0), pl.program_id(1)
    hd = qg_ref.shape[0]
    half = hd // 2
    heads_q, heads_k = heads
    cos_part, sin_part = cos_ref[...], sin_ref[...]
    tile = cos_part.shape[1]

    @pl.when((step == 0) & (part == 0))
    def _():
        gg_ref[...] = jnp.zeros_like(gg_ref)

    def work(d_ref, r_ref):
        gain_q = jnp.zeros((hd, 1), F32)
        gain_k = jnp.zeros((hd, 1), F32)
        done = []
        for h in range(heads_q + heads_k):
            is_q = h < heads_q
            g = d_ref[h * hd : (h + 1) * hd, :].astype(F32)
            raw = r_ref[h * hd : (h + 1) * hd, :].astype(F32)
            a, b = g[:half], g[half:]
            turned = jnp.concatenate(
                [a * cos_part + b * sin_part, b * cos_part - a * sin_part], axis=0
            )
            rho = lax.rsqrt(jnp.mean(raw * raw, axis=0, keepdims=True) + EPS)
            unit = raw * rho
            prod = turned * unit
            scaled = turned * (qg_ref[...] if is_q else kg_ref[...])
            mean = jnp.mean(scaled * unit, axis=0, keepdims=True)
            done.append(rho * (scaled - unit * mean))
            total = jnp.sum(prod, axis=1, keepdims=True)
            if is_q:
                gain_q = gain_q + total
            else:
                gain_k = gain_k + total
        done.append(d_ref[(heads_q + heads_k) * hd :, :].astype(F32))
        out_ref[0] = jnp.concatenate(done, axis=0).T.astype(BF16)
        lane = lax.broadcasted_iota(jnp.int32, gg_ref.shape, 1)
        gg_ref[...] += jnp.where(lane == 0, gain_q, jnp.where(lane == 1, gain_k, 0.0))

    @pl.when(step == 0)
    def _():
        work(dm_ref, rm_ref)

    @pl.when(step == 1)
    def _():
        work(dt_ref, rt_ref)


def head_back(info, grad_mine, grad_theirs, raw_mine, raw_theirs, cos_part, sin_part, gq, gk, heads):
    cols, tok = grad_mine.shape
    tile = min(512, tok)
    mine = pl.BlockSpec((cols, tile), lambda s, i, info: (0, jnp.where(s == 0, i, tok // tile - 1)))
    theirs = pl.BlockSpec((cols, tile), lambda s, i, info: (0, jnp.where(s == 0, 0, i)))
    tab = lambda a: pl.BlockSpec((a.shape[0], tile), lambda s, i, info: (0, i))
    const = lambda a: pl.BlockSpec(a.shape, lambda s, i, info: (0, 0))
    return pl.pallas_call(
        functools.partial(head_back_kernel, heads),
        grid_spec=pltpu.PrefetchScalarGridSpec(
            num_scalar_prefetch=1,
            grid=(2, tok // tile),
            in_specs=[
                mine,
                theirs,
                mine,
                theirs,
                tab(cos_part),
                tab(sin_part),
                const(gq),
                const(gk),
            ],
            out_specs=[
                pl.BlockSpec(
                    (1, tile, cols), lambda s, i, info: (jnp.bitwise_xor(info[2], s), i, 0)
                ),
                pl.BlockSpec((gq.shape[0], 128), lambda s, i, info: (0, 0)),
            ],
        ),
        out_shape=[shape_of((2, tok, cols), BF16), shape_of((gq.shape[0], 128), F32)],
        compiler_params=settings(2, 60),
        cost_estimate=cost(False),
        name="head_back",
    )(info, grad_mine, grad_theirs, raw_mine, raw_theirs, cos_part, sin_part, gq, gk)


def load_rows(info, mine_ref, got_ref, rows, sems):
    tok = mine_ref.shape[1]
    ctx = info[2]
    here = pl.multiple_of(ctx * tok, tok)
    there = pl.multiple_of((1 - ctx) * tok, tok)
    one = pltpu.make_async_copy(mine_ref, rows.at[:, pl.ds(here, tok)], sems.at[0])
    two = pltpu.make_async_copy(got_ref, rows.at[:, pl.ds(there, tok)], sems.at[1])
    one.start()
    two.start()
    one.wait()
    two.wait()


def keys_with_bias(keys, length):
    hd, slots = keys.shape
    pos = lax.broadcasted_iota(jnp.int32, (hd, slots), 1)
    row = lax.broadcasted_iota(jnp.int32, (hd, slots), 0)
    bias = jnp.where((row == 0) & (pos >= length), NEGATIVE, 0.0)
    return jnp.concatenate([keys.astype(F32), bias], axis=0).T.astype(BF16)


def query_with_one(pair):
    one_row = jnp.where(lax.broadcasted_iota(jnp.int32, pair.shape, 0) == 0, 1.0, 0.0)
    return jnp.concatenate([pair, one_row.astype(BF16)], axis=0)


def by_halves(left, right):
    half = left.shape[1] // 2
    return jnp.concatenate(
        [left[:, :half], right[:, :half], left[:, half:], right[:, half:]], axis=1
    )


def by_heads(both):
    quarter = both.shape[1] // 4
    part = lambda i: both[:, i * quarter : (i + 1) * quarter]
    return (
        jnp.concatenate([part(0), part(2)], axis=1),
        jnp.concatenate([part(1), part(3)], axis=1),
    )


def causal(scores):
    half = scores.shape[0]
    key_pos = lax.broadcasted_iota(jnp.int32, (half, half), 0)
    query_pos = lax.broadcasted_iota(jnp.int32, (half, half), 1)
    allowed = key_pos <= query_pos
    return jnp.where(jnp.concatenate([allowed, allowed], axis=1), scores, NEGATIVE)


def attn_fwd_kernel(
    width, hd, info, mine_ref, got_ref, keep_ref, send_ref, lse_ref, rows, key_rows, sems
):
    head, block = pl.program_id(0), pl.program_id(1)
    heads_k = pl.num_programs(0)
    scale = hd**-0.5 * LOG2E
    length = info[3]
    key_at = pl.multiple_of(heads_k * 2 * hd + head * hd, hd)
    value_at = pl.multiple_of(heads_k * 3 * hd + head * hd, hd)
    query_at = pl.multiple_of(head * 2 * hd, 2 * hd)

    @pl.when((head == 0) & (block == 0))
    def _():
        load_rows(info, mine_ref, got_ref, rows, sems)

    @pl.when(block == 0)
    def _():
        key_rows[...] = keys_with_bias(rows[pl.ds(key_at, hd), :], length)

    start = pl.multiple_of(block * width, width)
    both = rows[pl.ds(query_at, 2 * hd), pl.ds(start, width)]
    query = query_with_one(by_halves(both[:hd], both[hd:]))

    def tile(at, carried, diagonal):
        out, total = carried
        scores = dot(key_rows[pl.ds(at, width), :], query, 1, 0)
        if diagonal:
            key_pos = lax.broadcasted_iota(jnp.int32, (width, width), 0)
            query_pos = lax.broadcasted_iota(jnp.int32, (width, width), 1)
            allowed = key_pos <= query_pos
            allowed = by_halves(allowed, allowed)
            scores = jnp.where(allowed, scores, NEGATIVE)
        probs = jnp.exp2(scores * scale)
        total = total + jnp.sum(probs, axis=0, keepdims=True)
        out = out + dot(rows[pl.ds(value_at, hd), pl.ds(at, width)], probs.astype(BF16), 1, 0)
        return out, total

    carried = (jnp.zeros((hd, 2 * width), F32), jnp.zeros((1, 2 * width), F32))
    full = jnp.minimum(block, lax.div(length + width - 1, width))
    carried = lax.fori_loop(
        0, full, lambda j, c: tile(pl.multiple_of(j * width, width), c, False), carried
    )
    out, total = tile(start, carried, True)
    out = out * (1.0 / total)
    out = jnp.concatenate(by_heads(out), axis=0).T.astype(BF16)
    here = block // 2 == info[2]

    @pl.when(here)
    def _():
        keep_ref[...] = out

    @pl.when(jnp.logical_not(here))
    def _():
        send_ref[...] = out

    log_first, log_second = by_heads(jnp.log2(total))
    lse_ref[0, 0:1, :] = log_first
    lse_ref[0, 1:2, :] = log_second


def keep_block(i, info):
    return jnp.clip(i - 2 * info[2], 0, 1)


def send_block(i, info):
    return jnp.clip(i - 2 * (1 - info[2]), 0, 1)


def attn_fwd(info, mine, got, hd):
    cols, tok = mine.shape
    heads_k = cols // (4 * hd)
    width = tok // 2
    return pl.pallas_call(
        functools.partial(attn_fwd_kernel, width, hd),
        grid_spec=pltpu.PrefetchScalarGridSpec(
            num_scalar_prefetch=1,
            grid=(heads_k, 4),
            in_specs=[ANY, ANY],
            out_specs=[
                pl.BlockSpec((width, 2 * hd), lambda h, i, info: (keep_block(i, info), h)),
                pl.BlockSpec((width, 2 * hd), lambda h, i, info: (send_block(i, info), h)),
                pl.BlockSpec((1, 2, width), lambda h, i, info: (h, 0, i)),
            ],
            scratch_shapes=[
                pltpu.VMEM((cols, 2 * tok), BF16),
                pltpu.VMEM((2 * tok, 2 * hd), BF16),
                pltpu.SemaphoreType.DMA((2,)),
            ],
        ),
        out_shape=[
            shape_of((tok, heads_k * 2 * hd), BF16),
            shape_of((tok, heads_k * 2 * hd), BF16),
            shape_of((heads_k, 2, 2 * tok), F32),
        ],
        compiler_params=settings(2, 60),
        cost_estimate=cost(True),
        name="attn_fwd",
    )(info, mine, got)


def attn_bwd_kernel(
    width,
    hd,
    info,
    mine_ref,
    got_ref,
    ok_ref,
    os_ref,
    gk_ref,
    gs_ref,
    lse_ref,
    keep_ref,
    send_ref,
    rows,
    key_rows,
    value_rows,
    key_sum,
    value_sum,
    sems,
):
    head, block = pl.program_id(0), pl.program_id(1)
    heads_k = pl.num_programs(0)
    scale = hd**-0.5
    length = info[3]
    ctx = info[2]
    tok = keep_ref.shape[1]
    key_at = pl.multiple_of(heads_k * 2 * hd + head * hd, hd)
    value_at = pl.multiple_of(heads_k * 3 * hd + head * hd, hd)
    query_at = pl.multiple_of(head * 2 * hd, 2 * hd)

    @pl.when((head == 0) & (block == 0))
    def _():
        load_rows(info, mine_ref, got_ref, rows, sems)

    @pl.when(block == 0)
    def _():
        key_rows[...] = keys_with_bias(rows[pl.ds(key_at, hd), :], length)
        value_rows[...] = rows[pl.ds(value_at, hd), :].astype(F32).T.astype(BF16)
        key_sum[...] = jnp.zeros_like(key_sum)
        value_sum[...] = jnp.zeros_like(value_sum)

    start = pl.multiple_of(block * width, width)
    here = block // 2 == ctx

    def store_query(value):
        at = pl.ds(pl.multiple_of((block % 2) * width, width), width)

        @pl.when(here)
        def _():
            keep_ref[pl.ds(query_at, 2 * hd), at] = value

        @pl.when(jnp.logical_not(here))
        def _():
            send_ref[pl.ds(query_at, 2 * hd), at] = value

    @pl.when(block * width < length)
    def _():
        both = rows[pl.ds(query_at, 2 * hd), pl.ds(start, width)]
        pair = by_halves(both[:hd], both[hd:])
        query = query_with_one(pair)
        query_rows = pair.astype(F32).T.astype(BF16)
        grad_wide = jnp.where(here, gk_ref[...].astype(F32), gs_ref[...].astype(F32))
        out_wide = jnp.where(here, ok_ref[...].astype(F32), os_ref[...].astype(F32))
        grad_t = grad_wide.T
        prod = (grad_wide * out_wide).T
        grad = by_halves(grad_t[:hd], grad_t[hd:]).astype(BF16)
        half = width // 2
        grad_rows = jnp.concatenate(
            [
                grad_wide[:half, :hd],
                grad_wide[:half, hd:],
                grad_wide[half:, :hd],
                grad_wide[half:, hd:],
            ],
            axis=0,
        ).astype(BF16)
        delta = by_halves(
            jnp.sum(prod[:hd], axis=0, keepdims=True), jnp.sum(prod[hd:], axis=0, keepdims=True)
        )
        lse = by_halves(lse_ref[0, 0:1, :], lse_ref[0, 1:2, :])

        def terms(at, keys, first, mask):
            scores = dot(key_rows[pl.ds(at, keys), :], query[:, first:], 1, 0)
            if mask:
                part = causal(scores[:, :width])
                wide = scores.shape[1] > width
                scores = jnp.concatenate([part, scores[:, width:]], axis=1) if wide else part
            probs = jnp.exp2(scores * (scale * LOG2E) - lse[:, first:])
            grad_probs = dot(value_rows[pl.ds(at, keys), :], grad[:, first:], 1, 0)
            grad_scores = (probs * (grad_probs - delta[:, first:])).astype(BF16)
            value_sum[pl.ds(at, keys), :] += dot(probs.astype(BF16), grad_rows[first:], 1, 0)
            key_sum[pl.ds(at, keys), :] += dot(grad_scores, query_rows[first:], 1, 0)
            return dot(rows[pl.ds(key_at, hd), pl.ds(at, keys)], grad_scores, 1, 0)

        query_sum = lax.fori_loop(
            0,
            block,
            lambda j, s: s + terms(pl.multiple_of(j * width, width), width, 0, False),
            jnp.zeros((hd, 2 * width), F32),
        )
        query_sum = query_sum + terms(start, half, 0, True)
        later = terms(pl.multiple_of(start + half, half), half, width, True)
        query_sum = jnp.concatenate([query_sum[:, :width], query_sum[:, width:] + later], axis=1)
        store_query(jnp.concatenate(by_heads(query_sum * scale), axis=0).astype(BF16))

    @pl.when(block * width >= length)
    def _():
        store_query(jnp.zeros((2 * hd, width), BF16))

    @pl.when(block == 3)
    def _():
        for at, total in ((key_at, key_sum[...] * scale), (value_at, value_sum[...])):
            total = total.T.astype(BF16)
            left, right = total[:, :tok], total[:, tok:]

            @pl.when(ctx == 0)
            def _():
                keep_ref[pl.ds(at, hd), :] = left
                send_ref[pl.ds(at, hd), :] = right

            @pl.when(ctx == 1)
            def _():
                keep_ref[pl.ds(at, hd), :] = right
                send_ref[pl.ds(at, hd), :] = left


def attn_bwd(info, mine, got, out_keep, out_send, grad_keep, grad_send, lse, hd):
    cols, tok = mine.shape
    heads_k = cols // (4 * hd)
    width = tok // 2
    keep = pl.BlockSpec((width, 2 * hd), lambda h, i, info: (keep_block(i, info), h))
    send = pl.BlockSpec((width, 2 * hd), lambda h, i, info: (send_block(i, info), h))
    full = pl.BlockSpec((cols, tok), lambda h, i, info: (0, 0))
    return pl.pallas_call(
        functools.partial(attn_bwd_kernel, width, hd),
        grid_spec=pltpu.PrefetchScalarGridSpec(
            num_scalar_prefetch=1,
            grid=(heads_k, 4),
            in_specs=[
                ANY,
                ANY,
                keep,
                send,
                keep,
                send,
                pl.BlockSpec((1, 2, width), lambda h, i, info: (h, 0, i)),
            ],
            out_specs=[full, full],
            scratch_shapes=[
                pltpu.VMEM((cols, 2 * tok), BF16),
                pltpu.VMEM((2 * tok, 2 * hd), BF16),
                pltpu.VMEM((2 * tok, hd), BF16),
                pltpu.VMEM((2 * tok, hd), F32),
                pltpu.VMEM((2 * tok, hd), F32),
                pltpu.SemaphoreType.DMA((2,)),
            ],
        ),
        out_shape=[shape_of((cols, tok), BF16), shape_of((cols, tok), BF16)],
        compiler_params=settings(2, 60),
        cost_estimate=cost(True, 16.2),
        name="attn_bwd",
    )(info, mine, got, out_keep, out_send, grad_keep, grad_send, lse)


def load_blocks(plan, pieces, target, sem):
    rows = target.shape[1] // 4

    @pl.when(pl.program_id(0) == 0)
    def _():
        for k, places in enumerate(plan):
            for p, (piece, row) in enumerate(places):
                src = pieces[piece].at[pl.ds(row, rows)]
                pltpu.make_async_copy(src, target.at[k, pl.ds(p * rows, rows)], sem).start()
        pltpu.make_async_copy(target, target, sem).wait()


def out_proj_kernel(plan, count, info, *refs):
    x_ref, a0, a1, b0, b1, gain_ref, r_ref, n_ref, nt_ref, att_ref, w_ref, sem = refs[count:]
    load_blocks(plan, refs, w_ref, sem)
    ctx = info[2]
    total = x_ref[...].astype(F32)
    for j, ref, side in ((0, a0, ctx), (1, a1, ctx), (0, b0, 1 - ctx), (1, b1, 1 - ctx)):
        block = 2 * side + j
        part = ref[...]
        att_ref[block] = part
        total = total + dot(part, w_ref[block], 1, 1)
    rho = lax.rsqrt(jnp.mean(total * total, axis=-1, keepdims=True) + EPS)
    normed = total * rho * gain_ref[...]
    r_ref[...] = total
    n_ref[...] = normed.astype(BF16)
    nt_ref[...] = normed.T.astype(BF16)


def out_proj(info, x, mine, theirs, weights, gain, tile):
    plan, pieces = weights
    tok, width = x.shape
    feats = pieces[0].shape[1]
    rows_of = lambda n: pl.BlockSpec((tile, n), lambda i, info: (i, 0))
    return pl.pallas_call(
        functools.partial(out_proj_kernel, plan, len(pieces)),
        grid_spec=pltpu.PrefetchScalarGridSpec(
            num_scalar_prefetch=1,
            grid=(tok // tile,),
            in_specs=[ANY] * len(pieces)
            + [rows_of(width)]
            + [rows_of(feats)] * 4
            + [pl.BlockSpec((1, width), lambda i, info: (0, 0))],
            out_specs=[
                rows_of(width),
                rows_of(width),
                pl.BlockSpec((width, tile), lambda i, info: (0, i)),
                pl.BlockSpec((4, tile, feats), lambda i, info: (0, i, 0)),
            ],
            scratch_shapes=[pltpu.VMEM((4, width, feats), BF16), pltpu.SemaphoreType.DMA],
        ),
        out_shape=[
            shape_of((tok, width), F32),
            shape_of((tok, width), BF16),
            shape_of((width, tok), BF16),
            shape_of((4, tok, feats), BF16),
        ],
        compiler_params=settings(1, 60),
        cost_estimate=cost(True),
        name="out_proj",
    )(info, *pieces, x, *mine, *theirs, gain)


def norm_two_back_kernel(plan, count, info, *refs):
    g_ref, r_ref, gr_ref, gain_ref, gres_ref, gat_ref, a0, a1, b0, b1, gg_ref, w_ref, sem = refs[count:]
    load_blocks(plan, refs, w_ref, sem)
    ctx = info[2]
    grad, resid = g_ref[...], r_ref[...]
    rho = lax.rsqrt(jnp.mean(resid * resid, axis=-1, keepdims=True) + EPS)
    unit = resid * rho
    scaled = grad * gain_ref[...]
    back = rho * (scaled - unit * jnp.mean(scaled * unit, axis=-1, keepdims=True))
    total = gr_ref[...].astype(F32) + back
    low = total.astype(BF16)
    gres_ref[...] = low
    gat_ref[...] = total.T.astype(BF16)

    @pl.when(pl.program_id(0) == 0)
    def _():
        gg_ref[...] = jnp.zeros_like(gg_ref)

    gg_ref[...] += jnp.sum(grad * unit, axis=0, keepdims=True)
    for j, ref, side in ((0, a0, ctx), (1, a1, ctx), (0, b0, 1 - ctx), (1, b1, 1 - ctx)):
        ref[...] = dot(low, w_ref[2 * side + j], 1, 0).astype(BF16)


def norm_two_back(info, grad, resid, grad_result, gain, weights, tile):
    plan, pieces = weights
    tok, width = grad.shape
    feats = pieces[0].shape[1]
    rows_of = lambda n: pl.BlockSpec((tile, n), lambda i, info: (i, 0))
    row = pl.BlockSpec((1, width), lambda i, info: (0, 0))
    return pl.pallas_call(
        functools.partial(norm_two_back_kernel, plan, len(pieces)),
        grid_spec=pltpu.PrefetchScalarGridSpec(
            num_scalar_prefetch=1,
            grid=(tok // tile,),
            in_specs=[ANY] * len(pieces) + [rows_of(width)] * 3 + [row],
            out_specs=[rows_of(width), pl.BlockSpec((width, tile), lambda i, info: (0, i))]
            + [rows_of(feats)] * 4
            + [row],
            scratch_shapes=[pltpu.VMEM((4, width, feats), BF16), pltpu.SemaphoreType.DMA],
        ),
        out_shape=[shape_of((tok, width), BF16), shape_of((width, tok), BF16)]
        + [shape_of((tok, feats), BF16)] * 4
        + [shape_of((1, width), F32)],
        compiler_params=settings(1, 60),
        cost_estimate=cost(True, 5.4),
        name="norm_two_back",
    )(info, *pieces, grad, resid, grad_result, gain)


def norm_one_back_kernel(plan, count, info, *refs):
    p0, p1, x_ref, gres_ref, gain_ref, out_ref, gg_ref, w_ref, sem = refs[count:]
    load_blocks(plan, refs, w_ref, sem)
    quarter = x_ref.shape[1] // 4
    grad = dot(p0[0], w_ref[0], 1, 1)
    grad = grad + dot(p1[0], w_ref[1], 1, 1)
    grad = grad + dot(p0[1], w_ref[2], 1, 1)
    grad = grad + dot(p1[1], w_ref[3], 1, 1)
    x = x_ref[...].astype(F32)
    rho = lax.rsqrt(jnp.mean(x * x, axis=-1, keepdims=True) + EPS)
    unit = x * rho
    scaled = grad * gain_ref[...]
    back = rho * (scaled - unit * jnp.mean(scaled * unit, axis=-1, keepdims=True))
    total = (gres_ref[...].astype(F32) + back).astype(BF16)
    for p, mask in enumerate(MASKS):
        at = pl.multiple_of(jnp.bitwise_xor(info[1], mask) * quarter, quarter)
        part = total[:, p * quarter : (p + 1) * quarter]

        out_ref[:, pl.ds(at, quarter)] = part

    @pl.when(pl.program_id(0) == 0)
    def _():
        gg_ref[...] = jnp.zeros_like(gg_ref)

    gg_ref[...] += jnp.sum(grad * unit, axis=0, keepdims=True)


def norm_one_back(info, pairs, weights, x, grad_resid, gain, tile, part):
    plan, pieces = weights
    tok, width = x.shape
    cols = pieces[0].shape[1]
    steps = tok // tile // 2
    first = part * steps
    rows_of = lambda n: pl.BlockSpec((tile, n), lambda i, info: (first + i, 0))
    out_rows = pl.BlockSpec((tile, width), lambda i, info: (i, 0))
    pair = pl.BlockSpec((2, tile, cols), lambda i, info: (0, first + i, 0))
    row = pl.BlockSpec((1, width), lambda i, info: (0, 0))
    return pl.pallas_call(
        functools.partial(norm_one_back_kernel, plan, len(pieces)),
        grid_spec=pltpu.PrefetchScalarGridSpec(
            num_scalar_prefetch=1,
            grid=(steps,),
            in_specs=[ANY] * len(pieces) + [pair, pair, rows_of(width), rows_of(width), row],
            out_specs=[out_rows, row],
            scratch_shapes=[pltpu.VMEM((4, width, cols), BF16), pltpu.SemaphoreType.DMA],
        ),
        out_shape=[shape_of((tok // 2, width), BF16), shape_of((1, width), F32)],
        compiler_params=settings(1, 60),
        cost_estimate=cost(True),
        name="norm_one_back",
    )(info, *pieces, *pairs, x, grad_resid, gain)


def weight_copies(plan, pieces, gate_up, down, gate_up_sem, down_sem):
    third = down.shape[1] // 3
    rows = down.shape[0] // 4
    wide, thin = [], []
    for p, chunks in enumerate(plan):
        block = pl.ds(p * rows, rows)
        for j, (piece, row, at) in enumerate(chunks):
            src = pieces[piece].at[pl.ds(row, rows)]
            wide.append(
                pltpu.make_async_copy(
                    src.at[:, pl.ds(at, 2 * third)],
                    gate_up.at[block, pl.ds(j * 2 * third, 2 * third)],
                    gate_up_sem,
                )
            )
            thin.append(
                pltpu.make_async_copy(
                    src.at[:, pl.ds(at + 2 * third, third)],
                    down.at[block, pl.ds(j * third, third)],
                    down_sem,
                )
            )
    return wide, thin


def split_act(act):
    third = act.shape[1] // 6
    part = lambda j: act[:, j * third : (j + 1) * third]
    return [(part(0), part(1)), (part(2), part(3)), (part(4), part(5))]


def ffn_fwd_kernel(tile, plans, last, info, scale, x_ref, in_ref, *rest):
    if last:
        teach_ref, rest = rest[0], rest[1:]
    pieces = []
    for plan in plans:
        count = 1 + max(place[0] for chunks in plan for place in chunks)
        pieces.append(rest[:count])
        rest = rest[count:]
    act_ref, hid_ref = rest[:2]
    if last:
        out_ref, low_ref, lowt_ref, sq_ref = rest[2:6]
        gate_up, down, total, sems = rest[6:]
    else:
        sum_ref, gate_up, down, total, sems = rest[2:]
    step, part = pl.program_id(0), pl.program_id(1)
    final = len(plans) - 1
    width = x_ref.shape[1]
    quarter = width // 4
    third = down.shape[2] // 3

    def copies(s):
        return weight_copies(
            plans[s], pieces[s], gate_up.at[s], down.at[s], sems.at[s, 0], sems.at[s, 1]
        )

    @pl.when((step == 0) & (part == 0))
    def _():
        for s in range(len(plans)):
            wide, thin = copies(s)
            for copy in wide + thin:
                copy.start()

    for s in range(len(plans)):

        @pl.when((step == s) & (part == 0))
        def _():
            pltpu.make_async_copy(gate_up.at[s], gate_up.at[s], sems.at[s, 0]).wait()

    rows = pl.ds(pl.multiple_of(part * tile, tile), tile)
    act = dot(x_ref[rows, :], gate_up[step], 1, 0)
    for j, (gate, upper) in enumerate(split_act(act)):
        sig = sigmoid(gate)
        silu = gate * sig
        hid_ref[0, :, j * third : (j + 1) * third] = (silu * upper).astype(BF16)
        at = 2 * j * third
        act_ref[0, :, at : at + third] = (upper * (sig + silu - silu * sig)).astype(BF16)
        act_ref[0, :, at + third : at + 2 * third] = silu.astype(BF16)
    for s in range(len(plans)):

        @pl.when((step == s) & (part == 0))
        def _():
            pltpu.make_async_copy(down.at[s], down.at[s], sems.at[s, 1]).wait()

    grown = dot(hid_ref[0], down[step], 1, 1)

    @pl.when(step == 0)
    def _():
        total[rows, :] = in_ref[...] + grown

    @pl.when(step > 0)
    def _():
        total[rows, :] += grown

    @pl.when(step == final)
    def _():
        result = total[rows, :]
        if not last:
            sum_ref[...] = result
            return
        tok = x_ref.shape[0]
        slot = info[2] * tok + part * tile + lax.broadcasted_iota(jnp.int32, (tile, 1), 0)
        valid = jnp.where(slot < info[3], 1.0, 0.0)
        square = jnp.zeros((tile, quarter), F32)
        for p, mask in enumerate(MASKS):
            at = pl.multiple_of(jnp.bitwise_xor(info[1], mask) * quarter, quarter)
            cols = slice(p * quarter, (p + 1) * quarter)
            value = result[:, cols]
            out_ref[:, pl.ds(at, quarter)] = value.astype(BF16)
            error = valid * (value - teach_ref[0, :, pl.ds(at, quarter)].astype(F32))
            square = square + error * error
            grad = error * scale[0]
            low_ref[:, cols] = grad.astype(BF16)
            lowt_ref[cols, :] = grad.T.astype(BF16)

        @pl.when(part == 0)
        def _():
            sq_ref[...] = jnp.zeros_like(sq_ref)

        sq_ref[...] += jnp.sum(square, axis=0, keepdims=True)


def ffn_fwd(info, scale, x, total, teacher, weights, units, tile):
    tok, width = x.shape
    pieces = [piece for _, group in weights for piece in group]
    count = len(weights)
    last = teacher is not None
    entry = lambda s, i: jnp.where(s == 0, i, tok // tile - 1)
    leave = lambda s, i: jnp.where(s == count - 1, i, 0)
    tiles = lambda n: pl.BlockSpec((tile, n), lambda s, i, info: (leave(s, i), 0))
    slab = lambda n: pl.BlockSpec((1, tile, n), lambda s, i, info: (s, i, 0))
    in_specs = [
        SMEM,
        whole((tok, width)),
        pl.BlockSpec((tile, width), lambda s, i, info: (entry(s, i), 0)),
    ]
    out_specs = [slab(2 * units), slab(units)]
    out_shape = [shape_of((count, tok, 2 * units), BF16), shape_of((count, tok, units), BF16)]
    if last:
        in_specs.append(
            pl.BlockSpec((1, tile, width), lambda s, i, info: (info[0], leave(s, i), 0))
        )
        out_specs += [
            tiles(width),
            tiles(width),
            pl.BlockSpec((width, tile), lambda s, i, info: (0, leave(s, i))),
            pl.BlockSpec((1, width // 4), lambda s, i, info: (0, 0)),
        ]
        out_shape += [
            shape_of((tok, width), BF16),
            shape_of((tok, width), BF16),
            shape_of((width, tok), BF16),
            shape_of((1, width // 4), F32),
        ]
    else:
        out_specs.append(tiles(width))
        out_shape.append(shape_of((tok, width), F32))
    return pl.pallas_call(
        functools.partial(ffn_fwd_kernel, tile, [plan for plan, _ in weights], last),
        grid_spec=pltpu.PrefetchScalarGridSpec(
            num_scalar_prefetch=1,
            grid=(count, tok // tile),
            in_specs=in_specs + [ANY] * len(pieces),
            out_specs=out_specs,
            scratch_shapes=[
                pltpu.VMEM((count, width, 2 * units), BF16),
                pltpu.VMEM((count, width, units), BF16),
                pltpu.VMEM((tok, width), F32),
                pltpu.SemaphoreType.DMA((count, 2)),
            ],
        ),
        out_shape=out_shape,
        compiler_params=settings(2, 60),
        cost_estimate=cost(True),
        name="ffn_fwd",
    )(info, scale, x, total, *([teacher] if last else []), *pieces)


def ffn_bwd_kernel(steps, plan, first, low_ref, act_ref, hid_ref, xt_ref, lowt_ref, *rest):
    count = 1 + max(place[0] for chunks in plan for place in chunks)
    pieces, rest = rest[:count], rest[count:]
    if not first:
        in_ref, rest = rest[0], rest[1:]
    out_ref, keep_ref, send_ref, gate_up, down, dact_all, hid_all, sems = rest
    step = pl.program_id(0)
    units = down.shape[1]
    third = units // 3
    tile = low_ref.shape[0]

    @pl.when(step == 0)
    def _():
        wide, thin = weight_copies(plan, pieces, gate_up, down, sems.at[0], sems.at[1])
        for copy in thin + wide:
            copy.start()
        pltpu.make_async_copy(down, down, sems.at[1]).wait()

    @pl.when(step < steps)
    def _():
        rows = pl.ds(pl.multiple_of(step * tile, tile), tile)
        grad_hidden = dot(low_ref[...], down[...], 1, 0)
        for j, (to_gate, to_upper) in enumerate(split_act(act_ref[0])):
            grad = grad_hidden[:, j * third : (j + 1) * third]
            at = 2 * j * third
            dact_all[rows, at : at + third] = (grad * to_gate.astype(F32)).astype(BF16)
            dact_all[rows, at + third : at + 2 * third] = (grad * to_upper.astype(F32)).astype(BF16)
        hid_all[rows, :] = hid_ref[0]

        @pl.when(step == 0)
        def _():
            pltpu.make_async_copy(gate_up, gate_up, sems.at[0]).wait()

        grown = dot(dact_all[rows, :], gate_up[...], 1, 1)
        out_ref[...] = grown if first else in_ref[...] + grown

    def weight_rows(target):
        target[:, : 2 * units] = dot(xt_ref[...], dact_all[...], 1, 0).astype(BF16)
        target[:, 2 * units :] = dot(lowt_ref[...], hid_all[...], 1, 0).astype(BF16)

    @pl.when((step >= steps) & (step < steps + 2))
    def _():
        weight_rows(send_ref)

    @pl.when(step >= steps + 2)
    def _():
        weight_rows(keep_ref)


def ffn_bwd(low, saved, weights, total, xt, lowt, tile):
    plan, pieces = weights
    acts, hiddens, block = saved
    tok, width = low.shape
    units = hiddens.shape[2]
    steps = tok // tile
    quarter = width // 4
    first = total is None
    clip = lambda i: jnp.minimum(i, steps - 1)
    rows_of = lambda n: pl.BlockSpec((tile, n), lambda i: (clip(i), 0))
    slab = lambda n: pl.BlockSpec((1, tile, n), lambda i: (block, clip(i), 0))
    feature = lambda i: (jnp.where(i < steps + 2, jnp.maximum(i - steps, 0) + 2, i - steps - 2), 0)
    return pl.pallas_call(
        functools.partial(ffn_bwd_kernel, steps, plan, first),
        grid=(steps + 4,),
        in_specs=[
            rows_of(width),
            slab(2 * units),
            slab(units),
            pl.BlockSpec((quarter, tok), feature),
            pl.BlockSpec((quarter, tok), feature),
        ]
        + [ANY] * len(pieces)
        + ([] if first else [rows_of(width)]),
        out_specs=[
            rows_of(width),
            pl.BlockSpec((quarter, 3 * units), lambda i: (jnp.maximum(i - steps - 2, 0), 0)),
            pl.BlockSpec((quarter, 3 * units), lambda i: (jnp.clip(i - steps, 0, 1), 0)),
        ],
        out_shape=[
            shape_of((tok, width), F32),
            shape_of((width // 2, 3 * units), BF16),
            shape_of((width // 2, 3 * units), BF16),
        ],
        scratch_shapes=[
            pltpu.VMEM((width, 2 * units), BF16),
            pltpu.VMEM((width, units), BF16),
            pltpu.VMEM((tok, 2 * units), BF16),
            pltpu.VMEM((tok, units), BF16),
            pltpu.SemaphoreType.DMA((2,)),
        ],
        input_output_aliases={} if first else {5 + len(pieces): 0},
        compiler_params=settings(1, 60),
        cost_estimate=cost(True, 11.2),
        name="ffn_bwd",
    )(low, acts, hiddens, xt, lowt, *pieces, *([] if first else [total]))


def turn_chunks(block):
    wide = block.shape[1] * 2 // 9
    thin = wide // 2
    starts = [(2 * wide, wide), (wide, wide), (0, wide)]
    starts += [(3 * wide + 2 * thin, thin), (3 * wide + thin, thin), (3 * wide, thin)]
    return jnp.concatenate([block[:, a : a + n] for a, n in starts], axis=1)


def sum_kernel(turns, *refs):
    total = None
    for ref, turn in zip(refs[:-1], turns):
        value = ref[...].astype(F32)
        value = turn_chunks(value) if turn else value
        total = value if total is None else total + value
    refs[-1][...] = total.astype(refs[-1].dtype)


def summed(terms, turns=None, dtype=BF16):
    rows, cols = terms[0].shape
    spec = pl.BlockSpec((128, cols), lambda i: (i, 0))
    return pl.pallas_call(
        functools.partial(sum_kernel, turns or [False] * len(terms)),
        grid=(rows // 128,),
        in_specs=[spec] * len(terms),
        out_specs=spec,
        out_shape=shape_of((rows, cols), dtype),
        compiler_params=settings(1, 60),
        cost_estimate=cost(False),
        name="summed",
    )(*terms)


def sums_kernel(jobs, count, info, *refs):
    arrays, refs = refs[:count], refs[count:]
    outs, (term_buf, out_buf, term_sems, out_sems) = refs[: len(jobs)], refs[len(jobs) :]
    rows = term_buf.shape[1]
    copies = []
    for terms in jobs:
        group = []
        for array, base, pick, _ in terms:
            at = base
            if pick is not None:
                at = pl.multiple_of(base + jnp.bitwise_xor(info[2], pick) * rows, rows)
            i = len(copies) + len(group)
            src = arrays[array].at[pl.ds(at, rows)]
            group.append(pltpu.make_async_copy(src, term_buf.at[i], term_sems.at[i]))
            group[-1].start()
        copies += group
    first = 0
    stores = []
    for j, terms in enumerate(jobs):
        total = None
        for i, (_, _, _, turn) in enumerate(terms):
            copies[first + i].wait()
            value = term_buf[first + i].astype(F32)
            value = turn_chunks(value) if turn else value
            total = value if total is None else total + value
        first += len(terms)
        out_buf[j] = total.astype(BF16)
        stores.append(pltpu.make_async_copy(out_buf.at[j], outs[j], out_sems.at[j]))
        stores[-1].start()
    for store in stores:
        store.wait()


def sums(info, arrays, jobs):
    cols = arrays[0].shape[1]
    rows, terms = 128, sum(len(job) for job in jobs)
    return pl.pallas_call(
        functools.partial(sums_kernel, jobs, len(arrays)),
        grid_spec=pltpu.PrefetchScalarGridSpec(
            num_scalar_prefetch=1,
            grid=(1,),
            in_specs=[ANY] * len(arrays),
            out_specs=[ANY] * len(jobs),
            scratch_shapes=[
                pltpu.VMEM((terms, rows, cols), BF16),
                pltpu.VMEM((len(jobs), rows, cols), BF16),
                pltpu.SemaphoreType.DMA((terms,)),
                pltpu.SemaphoreType.DMA((len(jobs),)),
            ],
        ),
        out_shape=[shape_of((rows, cols), BF16)] * len(jobs),
        compiler_params=settings(1, 60),
        cost_estimate=cost(False),
        name="sums",
    )(info, *arrays)


def core_jobs(keep, came):
    return [[(a, far * 256, pick, False) for a in (keep, came)] for far in (0, 1) for pick in (0, 1)]


def core_sum_kernel(info, left_ref, right_ref, *outs):
    total = (left_ref[...].astype(F32) + right_ref[...].astype(F32)).astype(BF16)
    block = pl.program_id(1)
    place = block // 2 * 2 + jnp.bitwise_xor(block % 2, info[2])
    for i, out in enumerate(outs):

        @pl.when(place == i)
        def _():
            out[...] = total


def core_sum(info, keep, came):
    groups, rows, cols = keep.shape
    spec = pl.BlockSpec((1, rows // 4, cols), lambda g, i, info: (g, i, 0))
    return pl.pallas_call(
        core_sum_kernel,
        grid_spec=pltpu.PrefetchScalarGridSpec(
            num_scalar_prefetch=1,
            grid=(groups, 4),
            in_specs=[spec] * 2,
            out_specs=[pl.BlockSpec((1, rows // 4, cols), lambda g, i, info: (g, 0, 0))] * 4,
        ),
        out_shape=[shape_of((groups, rows // 4, cols), BF16)] * 4,
        compiler_params=settings(2, 24),
        cost_estimate=cost(False),
        name="core_sum",
    )(info, keep, came)


def weight_grad_kernel(nt_ref, back0_ref, back1_ref, gt_ref, att_ref, keep_ref, send_ref):
    cols = back0_ref.shape[2]
    part, block = pl.program_id(0), pl.program_id(1)

    def rows(target, back_ref):
        target[0, :, :cols] = dot(nt_ref[...], back_ref[0], 1, 0).astype(BF16)
        target[0, :, cols:] = dot(gt_ref[...], att_ref[0], 1, 0).astype(BF16)

    for j, back_ref in enumerate((back0_ref, back1_ref)):

        @pl.when((part == 0) & (block % 2 == j))
        def _():
            rows(send_ref, back_ref)

        @pl.when((part == 1) & (block % 2 == j))
        def _():
            rows(keep_ref, back_ref)


def weight_grad(normed_t, backs, grad_t, attended):
    width, tok = normed_t.shape
    cols, feats = backs[0].shape[2], attended.shape[2]
    half = pl.BlockSpec((width // 2, tok), lambda p, k: (1 - p, 0))
    side = pl.BlockSpec((1, tok, cols), lambda p, k: (k // 2, 0, 0))
    shape = (1, width // 2, cols + feats)
    return pl.pallas_call(
        weight_grad_kernel,
        grid=(2, 4),
        in_specs=[half, side, side, half, pl.BlockSpec((1, tok, feats), lambda p, k: (k, 0, 0))],
        out_specs=[
            pl.BlockSpec(shape, lambda p, k: (jnp.where(p == 0, 0, k), 0, 0)),
            pl.BlockSpec(shape, lambda p, k: (jnp.where(p == 0, k, 3), 0, 0)),
        ],
        out_shape=[shape_of((4, width // 2, cols + feats), BF16)] * 2,
        compiler_params=settings(2, 60),
        cost_estimate=cost(True),
        name="weight_grad",
    )(normed_t, *backs, grad_t, attended)


def copy_kernel(in_ref, out_ref):
    out_ref[...] = in_ref[...]


def copied(array):
    spec = pl.BlockSpec((1,) + array.shape[1:], lambda i: (i, 0, 0))
    return pl.pallas_call(
        copy_kernel,
        grid=(array.shape[0],),
        in_specs=[spec],
        out_specs=spec,
        out_shape=shape_of(array.shape, array.dtype),
        compiler_params=settings(1, 24),
        cost_estimate=cost(False),
        name="copied",
    )(array)


def after(value, *others):
    return lax.optimization_barrier((value,) + others)[0]


class Live:

    def update(self, **values):
        vars(self).update(values)


def per_device_rows(
    tokens,
    teacher,
    lengths,
    attn_gain,
    q_weight,
    k_weight,
    v_weight,
    q_gain,
    k_gain,
    o_weight,
    ffn_gain,
    gate_weight,
    up_weight,
    down_weight,
):
    z = lax.axis_index("tp")
    ctx = lax.axis_index("ctx")
    fsdp = lax.axis_index("fsdp")
    rows_dev, tok, width = tokens.shape
    quarter = width // 4
    hd = q_gain.shape[0] * 4
    q_cols, k_cols = q_weight.shape[1], k_weight.shape[1]
    proj = q_cols + 2 * k_cols
    heads = (q_cols // hd, k_cols // hd)
    units = gate_weight.shape[1]
    slots = rows_dev * 4 * tok * 2

    def x_swap(v):
        return lax.ppermute(v, "fsdp", X_SWAP)

    def core_swap(v):
        return lax.ppermute(v, "fsdp", CORE_SWAP)

    def y_swap(v):
        return lax.ppermute(v, "ctx", Y_SWAP)

    def z_up(v):
        return lax.ppermute(v, "tp", Z_UP)

    def z_far(v):
        return lax.ppermute(v, "tp", Z_FAR)

    def z_down(v):
        return lax.ppermute(v, "tp", Z_DOWN)

    def natural(v):
        v = jnp.concatenate([v[0:1], v[2:3], v[1:2], v[3:4]], axis=0)
        v = jnp.where(fsdp % 2 == 0, v, jnp.concatenate([v[1:2], v[0:1], v[3:4], v[2:3]], axis=0))
        return jnp.where(fsdp // 2 == 0, v, jnp.concatenate([v[2:4], v[0:2]], axis=0))

    v = Live()

    def sync():
        v.update(**lax.optimization_barrier(dict(vars(v))))

    length = lax.dynamic_slice_in_dim(lengths, z, 1, 0)
    info = jnp.concatenate([jnp.stack([z, fsdp, ctx]).astype(jnp.int32), length])
    w_proj = join(q_weight, k_weight, v_weight)
    proj_z = [z_up(w_proj), z_far(w_proj), z_down(w_proj)]
    proj_own = jnp.concatenate([w_proj, x_swap(w_proj)], axis=0)
    count_here = jnp.sum(lengths).astype(F32)[None]
    vector = jnp.concatenate([attn_gain, ffn_gain, q_gain, k_gain]).astype(F32)
    vector = jnp.concatenate([vector, count_here, jnp.zeros((640 - 545,), F32)])[None]
    vector = jnp.concatenate([vector, x_swap(vector)], axis=0)
    vector = jnp.concatenate([vector, core_swap(vector)], axis=0)
    w_out, w_ffn, *w_chunks = pack(info, o_weight, gate_weight, up_weight, down_weight)
    pos = (ctx * tok + jnp.arange(tok, dtype=jnp.int32)).astype(F32)
    frequency = THETA ** (-(2.0 * jnp.arange(hd // 2, dtype=F32)) / hd)
    angles = frequency[:, None] * pos[None, :]
    head_gains = natural(vector[:, 2 * quarter : 544])
    v.update(
        info=info,
        proj_own=proj_own,
        proj_z=jnp.concatenate(proj_z, axis=0),
        w_out=w_out,
        w_ffn=w_ffn,
        w_chunks=w_chunks,
        gain_one=vector[:, :quarter].reshape(1, width),
        gain_two=vector[:, quarter : 2 * quarter].reshape(1, width),
        total_count=jnp.sum(vector[:, 544]),
        gain_q=head_gains[:, : hd // 4].reshape(hd, 1),
        gain_k=head_gains[:, hd // 4 :].reshape(hd, 1),
        cos_part=jnp.cos(angles),
        sin_part=jnp.sin(angles),
    )
    sync()
    info = v.info

    proj_zfar = x_swap(v.proj_z)
    out_z = [z_up(v.w_out), z_far(v.w_out), z_down(v.w_out)]
    own_core = core_swap(v.proj_own)
    x_in, normed_one_t = norm_one(info, tokens, v.gain_one, 256)
    v.update(
        proj_zfar=proj_zfar, own_core=own_core, x_in=x_in, normed_one_t=normed_one_t, out_z=out_z
    )
    sync()

    plan_proj = [[(0, 0), (0, quarter), (3, 0), (3, quarter)]]
    plan_proj += [[(p, k * quarter) for p in (1, 2, 4, 5)] for k in range(3)]
    weights_proj = [v.proj_own, v.proj_z, v.proj_zfar, v.own_core]
    weights_proj += [core_swap(v.proj_z), core_swap(v.proj_zfar)]
    one = [z_up(v.w_chunks[0]), z_up(v.w_chunks[3])]
    ffn_far = x_swap(v.w_ffn)
    tables = [v.cos_part, v.sin_part, v.gain_q, v.gain_k]

    def make(block, *then):
        normed_t = after(v.normed_one_t, *then)
        return project(info, (plan_proj, weights_proj), normed_t, *tables, heads, block)

    theirs = [make(lambda s: 2 * (1 - s[2]))]
    got = [y_swap(theirs[0][0])]
    theirs.append(make(lambda s: 2 * (1 - s[2]) + 1, theirs[0][0]))
    got.append(y_swap(theirs[1][0]))
    mine = [make(lambda s: 2 * s[2], theirs[1][0])]
    mine.append(make(lambda s: 2 * s[2] + 1, mine[0][0]))
    v.update(
        one=one,
        ffn_far=ffn_far,
        weights_proj=weights_proj,
        mine=mine,
        theirs=theirs,
        got0=got[0],
    )
    sync()

    one_far = [x_swap(v.one[0])]
    three = [z_down(v.w_chunks[0])]
    own_cores = [core_swap(v.w_ffn), core_swap(v.ffn_far)]
    first = attn_fwd(info, v.mine[0][0], v.got0, hd)
    v.update(first=first, got1=got[1], one_far=one_far, three=three, own_cores=own_cores)
    sync()

    arrived = [y_swap(v.first[1])]
    three = v.three + [z_down(v.w_chunks[1])]
    out_blocks = jnp.concatenate([v.w_out] + v.out_z, axis=0)
    out_far = x_swap(out_blocks)
    one_cores = [core_swap(v.one[0]), core_swap(v.one_far[0])]
    second = attn_fwd(info, v.mine[1][0], v.got1, hd)
    v.update(
        second=second,
        arrived=arrived,
        three=three,
        out_blocks=out_blocks,
        out_far=out_far,
        one_cores=one_cores,
    )
    sync()

    arrived = v.arrived + [y_swap(v.second[1])]
    three = v.three + [z_down(v.w_chunks[2])]
    one_far = v.one_far + [x_swap(v.one[1][:, :units])]
    weights_out = [v.out_blocks, v.out_far]
    weights_out += [core_swap(v.out_blocks), core_swap(v.out_far)]
    v.update(arrived=arrived, three=three, one_far=one_far, weights_out=weights_out)
    sync()

    plan_out = [[(p, k * quarter) for p in range(4)] for k in range(4)]
    two = [z_up(v.one[0])]
    three_far = [x_swap(v.three[0])]
    one_far = v.one_far + [y_swap(v.one_far[0])]
    one_cores = v.one_cores + [core_swap(v.one[1]), core_swap(v.one_far[1])]
    resid, normed_two, normed_two_t, attended = out_proj(
        info,
        v.x_in,
        [v.first[0], v.second[0]],
        v.arrived,
        (plan_out, v.weights_out),
        v.gain_two,
        256,
    )
    v.update(
        two=two,
        three_far=three_far,
        one_far=one_far,
        one_cores=one_cores,
        resid=resid,
        normed_two=normed_two,
        normed_two_t=normed_two_t,
        attended=attended,
    )
    sync()

    plan0 = [[(i, 0, j * units) for j in range(3)] for i in range(4)]
    plan_mixed = [[(0, 0, 0), (1, 0, 0), (1, 0, units)], [(i, 0, 0) for i in (2, 3, 4)]]
    plan_mixed += [[(5, 0, 0), (6, 0, 0), (6, 0, units)], [(i, 0, 0) for i in (7, 8, 9)]]
    scale = (slots / v.total_count)[None]
    weights0 = [v.w_ffn, v.ffn_far] + v.own_cores
    c0, cf, c1, cb = v.one_cores
    weights1 = v.one + v.one_far + [c0, c1, cf, cb, core_swap(v.one_far[2])]
    two = v.two + [z_up(v.one[1])]
    three_far = v.three_far + [x_swap(v.three[1]), y_swap(v.three_far[0])]
    two_far = [x_swap(v.two[0])]
    three_cores = [core_swap(v.three[0])]
    acts_a, hiddens_a, sum_a = ffn_fwd(
        info,
        scale,
        v.normed_two,
        v.resid,
        None,
        [(plan0, weights0), (plan_mixed, weights1)],
        units,
        256,
    )
    v.update(
        scale=scale,
        weights0=weights0,
        weights1=weights1,
        two=two,
        three_far=three_far,
        two_far=two_far,
        three_cores=three_cores,
        acts_a=acts_a,
        hiddens_a=hiddens_a,
        sum_a=sum_a,
    )
    sync()

    plan_chunks = [[(3 * p + j, 0, 0) for j in range(3)] for p in range(4)]
    weights3 = v.three + v.three_far + v.three_cores
    weights3 += [core_swap(part) for part in v.three[1:]]
    weights3 += [core_swap(part) for part in v.three_far]
    two_far = v.two_far + [x_swap(v.two[1][:, :units]), y_swap(v.two_far[0])]
    two_cores = [core_swap(part) for part in v.two + v.two_far]
    acts_b, hiddens_b, sum_b = ffn_fwd(
        info, v.scale, v.normed_two, v.sum_a, None, [(plan_chunks, weights3)], units, 256
    )
    v.update(
        weights3=weights3,
        two_far=two_far,
        two_cores=two_cores,
        acts_b=acts_b,
        hiddens_b=hiddens_b,
        sum_b=sum_b,
    )
    sync()

    weights2 = v.two + v.two_far + v.two_cores
    weights2 += [core_swap(part) for part in v.two_far[1:]]
    acts_c, hiddens_c, result_low, grad_low, grad_low_t, square = ffn_fwd(
        info, v.scale, v.normed_two, v.sum_b, teacher, [(plan_mixed, weights2)], units, 256
    )
    v.update(
        weights2=weights2,
        acts_c=acts_c,
        hiddens_c=hiddens_c,
        result_low=result_low,
        grad_low=grad_low,
        grad_low_t=grad_low_t,
        square=square,
    )
    sync()

    def ffn_back(plan, weights, acts, hiddens, block, total):
        return ffn_bwd(
            v.grad_low,
            (acts, hiddens, block),
            (plan, weights),
            total,
            v.normed_two_t,
            v.grad_low_t,
            256,
        )

    turned = [False, False, True]
    output = lax.all_gather(v.result_low, "tp", axis=0, tiled=False)
    total, keep2, send2 = ffn_back(plan_mixed, v.weights2, v.acts_c, v.hiddens_c, 0, None)
    v.update(total=total, keep2=keep2, send2=send2)
    sync()

    came2 = core_swap(v.send2)
    total, keep1, send1 = ffn_back(plan_mixed, v.weights1, v.acts_a, v.hiddens_a, 1, v.total)
    v.update(came2=came2, total=total, keep1=keep1, send1=send1)
    sync()

    came1 = core_swap(v.send1)
    sum2 = sums(info, [v.keep2, v.came2], core_jobs(0, 1))
    far_t2 = x_swap(sum2[3])
    total, keep3, send3 = ffn_back(
        plan_chunks, v.weights3, v.acts_b, v.hiddens_b, 0, after(v.total, sum2[0])
    )
    v.update(
        came1=came1,
        sum2=sum2,
        far_t2=far_t2,
        total=total,
        keep3=keep3,
        send3=send3,
    )
    sync()

    came3 = core_swap(v.send3)
    far_h2 = x_swap(v.sum2[2])
    there2, *sum1 = sums(
        info,
        [v.sum2[1], v.far_t2, v.keep1, v.came1],
        [[(0, 0, None, False), (1, 0, None, False)]] + core_jobs(2, 3),
    )
    there2 = y_swap(there2)
    total, keep0, send0 = ffn_back(
        plan0, v.weights0, v.acts_a, v.hiddens_a, 0, after(v.total, sum1[0])
    )
    v.update(
        came3=came3,
        far_h2=far_h2,
        there2=there2,
        sum1=sum1,
        total=total,
        keep0=keep0,
        send0=send0,
    )
    sync()

    came0 = core_swap(v.send0)
    far_t1 = x_swap(v.sum1[3])
    plane = [(0, 0, None, False), (1, 0, None, False), (2, 0, None, True)]
    part2, *sum3 = sums(
        info,
        [v.sum2[0], v.far_h2, v.there2, v.keep3, v.came3],
        [plane] + core_jobs(3, 4),
    )
    down2 = z_down(part2)
    grad_resid, grad_attn_t, a0, a1, b0, b1, gain_two_sum = norm_two_back(
        info,
        after(v.total, sum3[0]),
        v.resid,
        v.grad_low,
        v.gain_two,
        (plan_out, v.weights_out),
        256,
    )
    grad_got = [y_swap(b0), y_swap(b1)]
    v.update(
        came0=came0,
        far_t1=far_t1,
        sum3=sum3,
        grad_resid=grad_resid,
        grad_attn_t=grad_attn_t,
        grad_mine=[a0, a1],
        gain_two_sum=gain_two_sum,
    )
    sync()

    def attn_back(j, grad):
        out = (v.first, v.second)[j]
        got_ref = (v.got0, v.got1)[j]
        arrived = (v.grad_got0, grad_got[1] if j == 0 else v.grad_got1)[j]
        return attn_bwd(
            info, v.mine[j][0], got_ref, out[0], out[1], grad, arrived, out[2], hd
        )

    far_h1 = x_swap(v.sum1[2])
    there1, *sum0 = sums(
        info,
        [v.sum1[1], v.far_t1, v.keep0, v.came0],
        [[(0, 0, None, False), (1, 0, None, False)]] + core_jobs(2, 3),
    )
    there1 = y_swap(there1)
    far_t3 = x_swap(v.sum3[3])
    v.update(grad_got0=grad_got[0])
    back0 = attn_back(0, after(v.grad_mine[0], sum0[0]))
    v.update(
        far_h1=far_h1,
        there1=there1,
        far_t3=far_t3,
        down2=down2,
        sum0=sum0,
        back0=back0,
        grad_got1=grad_got[1],
    )
    sync()

    heads0 = y_swap(v.back0[1])
    far_h3 = x_swap(v.sum3[2])
    far_t0 = x_swap(v.sum0[3])
    [there3] = sums(info, [v.sum3[1], v.far_t3], [[(0, 0, None, False), (1, 0, None, False)]])
    there3_got = y_swap(there3)
    back1 = attn_back(1, after(v.grad_mine[1], there3, output))
    v.update(
        heads0=heads0, far_h3=far_h3, far_t0=far_t0, there3=there3_got, back1=back1
    )
    sync()

    heads1 = y_swap(v.back1[1])
    far_h0 = x_swap(v.sum0[2])
    part3, two_down, there0 = sums(
        info,
        [
            v.sum3[0],
            v.far_h3,
            v.there3,
            v.sum1[0],
            v.far_h1,
            v.there1,
            v.down2,
            v.sum0[1],
            v.far_t0,
        ],
        [
            plane,
            [(3, 0, None, False), (4, 0, None, False), (5, 0, None, True), (6, 0, None, False)],
            [(7, 0, None, False), (8, 0, None, False)],
        ],
    )
    two_down_got = z_down(two_down)
    up3 = z_up(part3)
    tables = [v.cos_part, v.sin_part, v.gain_q, v.gain_k]
    head0 = head_back(
        info, v.back0[0], v.heads0, v.mine[0][1], v.theirs[0][1], *tables, heads
    )
    v.update(heads1=heads1, head0=head0, there0=there0)
    sync()

    there0 = y_swap(v.there0)
    head1 = head_back(
        info, v.back1[0], v.heads1, v.mine[1][1], v.theirs[1][1], *tables, heads
    )
    def last_norm(part, *then):
        return norm_one_back(
            info,
            [v.head0[0], after(head1[0], *then)],
            (plan_proj, v.weights_proj),
            v.x_in,
            v.grad_resid,
            v.gain_one,
            tok // 4,
            part,
        )

    low_first, gain_first = last_norm(0)
    low_second, gain_second = last_norm(1, low_first)
    gathered = [lax.all_gather(low_first, "tp", axis=0, tiled=False)]
    tokens_low, gain_one_sum = low_second, gain_first + gain_second
    v.update(head1=head1, tokens_low=tokens_low, gain_one_sum=gain_one_sum, up3=up3)
    v.update(there0=there0, far_h0=far_h0, two_down=two_down_got)
    sync()

    gathered.append(lax.all_gather(v.tokens_low, "tp", axis=0, tiled=False))
    keep, send = weight_grad(
        v.normed_one_t, [v.head0[0], v.head1[0]], v.grad_attn_t, v.attended
    )
    gain_heads = v.head0[1] + v.head1[1]
    vector = jnp.concatenate(
        [
            natural(v.gain_one_sum.reshape(4, quarter)).reshape(1, width),
            natural(v.gain_two_sum.reshape(4, quarter)).reshape(1, width),
            gain_heads[:, 0].reshape(1, hd),
            gain_heads[:, 1].reshape(1, hd),
            jnp.sum(v.square).reshape(1, 1),
            jnp.zeros((1, 127), F32),
        ],
        axis=1,
    )
    vector = vector + core_swap(vector)
    v.update(keep=keep, send=send)
    v.update(vector=vector)
    sync()

    rows = quarter // 2
    flat = lambda a: a.reshape(4 * rows, a.shape[-1])
    attn_sums = [flat(p) for p in core_sum(info, v.keep, core_swap(v.send))]
    vector = v.vector + x_swap(v.vector)
    v.update(sums=attn_sums, vector=vector)
    sync()

    far_t = x_swap(v.sums[3])
    part0 = summed([v.sum0[0], v.far_h0, v.there0], turned)
    ffn_sum = summed([part0, v.two_down, v.up3], None, F32)
    vector = v.vector + y_swap(v.vector)
    v.update(far_t=far_t, ffn_sum=ffn_sum, vector=vector)
    sync()

    far_h = x_swap(v.sums[2])
    there = y_swap(summed([v.sums[1], v.far_t]))
    spread = copied(output)
    v.update(far_h=far_h, there=there, spread=spread)
    sync()

    parts = summed([v.sums[0], v.far_h, v.there])
    parts = [parts[k * rows : (k + 1) * rows] for k in range(4)]
    parts = [parts[0], z_down(parts[1]), z_far(parts[2]), z_up(parts[3])]
    ffn_other = y_swap(v.ffn_sum)
    v.update(parts=parts)
    sync()

    attn_sum = summed(v.parts, None, F32)
    vector = v.vector + lax.ppermute(v.vector, "tp", Z_NEAR)
    v.update(attn_sum=attn_sum, vector=vector)
    v.update(ffn_other=ffn_other)
    sync()

    def finish(own, other):
        return jnp.concatenate(
            [jnp.where(ctx == 0, own, other), jnp.where(ctx == 0, other, own)], axis=0
        )

    def columns(first):
        parts = [ffn_grad[:, first(j) : first(j) + third] for j in range(3)]
        return jnp.concatenate(
            [
                jnp.where(ctx == 0, parts[0], parts[2]),
                parts[1],
                jnp.where(ctx == 0, parts[2], parts[0]),
            ],
            axis=1,
        )

    attn_other = y_swap(v.attn_sum)
    vector = v.vector + lax.ppermute(v.vector, "tp", Z_FAR)
    third = units // 3
    ffn_grad = finish(v.ffn_sum, turn_chunks(v.ffn_other))
    grad_gate = columns(lambda j: 2 * j * third)
    grad_up = columns(lambda j: (2 * j + 1) * third)
    grad_down = columns(lambda j: 2 * units + j * third).T
    grad = jnp.zeros((rows_dev, tok, width), F32)
    grad = lax.dynamic_update_slice(grad, gathered[0].astype(F32), (0, 0, 0))
    v.update(vector=vector, attn_other=attn_other, grad=grad)
    v.update(grad_gate=grad_gate, grad_up=grad_up, grad_down=grad_down)
    sync()

    tokens_grad = lax.dynamic_update_slice(v.grad, gathered[1].astype(F32), (0, tok // 2, 0))
    sums_all = v.vector[0]

    attn_grad = finish(v.attn_sum, v.attn_other)
    teacher_loss = sums_all[2 * width + 2 * hd] / (v.total_count * width)

    def own_part(at, size):
        return lax.dynamic_slice_in_dim(sums_all, at + fsdp * (size // 4), size // 4, 0)

    return (
        v.spread,
        teacher_loss,
        tokens_grad,
        own_part(0, width),
        attn_grad[:, :q_cols],
        attn_grad[:, q_cols : q_cols + k_cols],
        attn_grad[:, q_cols + k_cols : proj],
        own_part(2 * width, hd),
        own_part(2 * width + hd, hd),
        attn_grad[:, proj:].T,
        own_part(width, width),
        v.grad_gate,
        v.grad_up,
        v.grad_down,
    )


def solution(mesh):
    return jax.shard_map(
        per_device_rows if fits(mesh) else per_device_any,
        mesh=mesh,
        in_specs=(
            P("fsdp", "ctx", None),
            P("fsdp", "ctx", None),
            P("fsdp"),
            P("fsdp"),
            P("fsdp", "tp"),
            P("fsdp", "tp"),
            P("fsdp", "tp"),
            P("fsdp"),
            P("fsdp"),
            P("tp", "fsdp"),
            P("fsdp"),
            P("fsdp", "tp"),
            P("fsdp", "tp"),
            P("tp", "fsdp"),
        ),
        out_specs=(
            P("fsdp", "ctx", None),
            P(),
            P("fsdp", "ctx", None),
            P("fsdp"),
            P("fsdp", "tp"),
            P("fsdp", "tp"),
            P("fsdp", "tp"),
            P("fsdp"),
            P("fsdp"),
            P("tp", "fsdp"),
            P("fsdp"),
            P("fsdp", "tp"),
            P("fsdp", "tp"),
            P("tp", "fsdp"),
        ),
        check_vma=False,
    )
```
